32 devices in a mesh: stream: 4 (over z), tm: 8 (over y, x, core).
Axes of the slice: x: 2, y: 2, z: 4, core: 2. Of those that a mesh axis runs over, the one named last changes fastest.
Arguments:
- frames: bfloat16 [4, 1024, 512], P('stream', 'tm'), may hold values from -6 to 6
- lengths: int32 [4, 5], P('stream'), may hold values from 1 to 896, as said below
- cotangent: bfloat16 [4, 1024, 512], P('stream', 'tm'), may hold values from -6 to 6
- ln_attn_gain: bfloat16 [512], replicated, may hold values from 0.25 to 1.75
- ln_attn_bias: bfloat16 [512], replicated, may hold values from -3 to 3
- ln_mlp_gain: bfloat16 [512], replicated, may hold values from 0.25 to 1.75
- ln_mlp_bias: bfloat16 [512], replicated, may hold values from -3 to 3
- qkv_weight: bfloat16 [512, 1536], replicated, may hold values from -0.25 to 0.25
- content_bias: bfloat16 [512], replicated, may hold values from -3 to 3
- position_bias: bfloat16 [512], replicated, may hold values from -3 to 3
- pos_weight: bfloat16 [512, 512], replicated, may hold values from -0.75 to 0.75
- out_weight: bfloat16 [512, 512], replicated, may hold values from -2 to 2
- up_weight: bfloat16 [512, 3072], replicated, may hold values from -0.25 to 0.25
- up_bias: bfloat16 [3072], replicated, may hold values from -3 to 3
- gate_norm_gain: bfloat16 [1536], replicated, may hold values from 0.25 to 1.75
- gate_norm_bias: bfloat16 [1536], replicated, may hold values from -3 to 3
- conv_kernel: bfloat16 [31, 1536], replicated, may hold values from -1 to 1
- conv_bias: bfloat16 [1536], replicated, may hold values from -3 to 3
- down_weight: bfloat16 [1536, 512], replicated, may hold values from -0.15625 to 0.15625
- down_bias: bfloat16 [512], replicated, may hold values from -2 to 2
- merge_weight: bfloat16 [1024, 512], replicated, may hold values from -0.1875 to 0.1875
- merge_bias: bfloat16 [512], replicated, may hold values from -3 to 3
Outputs:
- output: bfloat16 [4, 1024, 512], P('stream', 'tm')
- grad_frames: float32 [4, 1024, 512], P('stream', 'tm')
- grad_ln_attn_gain: float32 [512], P('stream')
- grad_ln_attn_bias: float32 [512], P('stream')
- grad_ln_mlp_gain: float32 [512], P('stream')
- grad_ln_mlp_bias: float32 [512], P('stream')
- grad_qkv_weight: float32 [512, 1536], P('stream')
- grad_content_bias: float32 [512], P('stream')
- grad_position_bias: float32 [512], P('stream')
- grad_pos_weight: float32 [512, 512], P('stream')
- grad_out_weight: float32 [512, 512], P('stream')
- grad_up_weight: float32 [512, 3072], P('stream')
- grad_up_bias: float32 [3072], P('stream')
- grad_gate_norm_gain: float32 [1536], P('stream')
- grad_gate_norm_bias: float32 [1536], P('stream')
- grad_conv_kernel: float32 [31, 1536], P(None, 'stream')
- grad_conv_bias: float32 [1536], P('stream')
- grad_down_weight: float32 [1536, 512], P('stream')
- grad_down_bias: float32 [512], P('stream')
- grad_merge_weight: float32 [1024, 512], P('stream')
- grad_merge_bias: float32 [512], P('stream')
The draws below stay inside these ranges and needn't reach their ends.
Inputs may be any that keep to these rules, and one draw needn't show every extreme that they name: Each stream's utterances start at frame 0 and lie end to end in order; exactly one of them, at a position that differs between streams, is 896 frames long, the others 1 to 32 frames; their lengths sum to at most 1024, the frames after them are padding.
All inputs are finite; a program needn't handle non-finite values.
Results may differ from the reference program's by a relative error of at most 0.025.
Values may be sent and summed in bfloat16 or wider, within the bound.
No kernel may reach another device: no remote copies, remote signals or barrier semaphores. Data moves between devices by JAX's collectives and lax.ppermute only.
A program may use at most 192 MiB of HBM per device.

```python
import math
import jax
import jax.numpy as jnp
from jax import lax

D = 512
HEADS = 8
HEAD = 64
FF = 3072
KERNEL = 31
TOK_DEV = 128
ITEMS = 5
HALF = 1536
FRAMES = 1024
STREAMS = 4


def draw_lengths(key, part):
    key = jax.random.fold_in(key, 7)
    first_key, second_key, place_key = jax.random.split(key, 3)
    quarter = TOK_DEV // 4
    first_factor = jax.random.randint(first_key, (STREAMS, ITEMS), 0, quarter).astype(jnp.int32)
    second_factor = jax.random.randint(second_key, (STREAMS, ITEMS), 0, quarter).astype(jnp.int32)
    short_items = (1 + first_factor * second_factor // quarter).astype(jnp.int32)
    long_place = jax.random.randint(place_key, (STREAMS, 1), 0, ITEMS).astype(jnp.int32)
    slots = jnp.arange(ITEMS, dtype=jnp.int32)[None, :]
    return jnp.where(slots == long_place, FRAMES - TOK_DEV, short_items).astype(jnp.int32)


def steps_of(own_key, shape, cuts, low, top_value):
    loudness = 1.0
    for dim, parts in cuts:
        draws = jax.random.uniform(jax.random.fold_in(jax.random.fold_in(own_key, 6), dim), (parts,), jnp.float32, low / len(cuts), top_value / len(cuts))
        loudness = loudness * jnp.repeat(jnp.exp(draws), shape[dim] // parts).reshape((-1,) + (1,) * (len(shape) - 1 - dim))
    return loudness


def gaussian(rng, extent, scale, limit, shards=(), kind=jnp.bfloat16):
    gain = steps_of(rng, extent, shards, -0.22, 0.18) if shards else 1.0
    entries = jax.random.normal(rng, extent, jnp.float32) * scale * gain
    return jnp.minimum(jnp.maximum(entries, -limit), limit).astype(kind)


def setup_inputs(seed: int = 0) -> dict:
    seeds = jax.random.split(jax.random.key(seed), 23)
    frames = gaussian(seeds[0], (STREAMS, FRAMES, D), 1.0, 6.0, ((0, 4), (1, 8)))
    lengths = draw_lengths(jax.random.fold_in(seeds[22], 71), 0)
    cotangent = gaussian(seeds[2], (STREAMS, FRAMES, D), 1.0, 6.0, ((0, 4), (1, 8)))
    ln_attn_gain = jnp.clip(1.0 + 0.15 * jax.random.normal(seeds[3], (D,), jnp.float32), 0.25, 1.75).astype(jnp.bfloat16)
    ln_attn_bias = gaussian(seeds[4], (D,), 0.5, 3.0)
    ln_mlp_gain = jnp.clip(1.0 + 0.15 * jax.random.normal(seeds[5], (D,), jnp.float32), 0.25, 1.75).astype(jnp.bfloat16)
    ln_mlp_bias = gaussian(seeds[6], (D,), 0.5, 3.0)
    qkv_weight = gaussian(seeds[7], (D, 3 * D), D ** -0.5, 0.25)
    content_bias = gaussian(seeds[8], (D,), 0.5, 3.0)
    position_bias = gaussian(seeds[9], (D,), 0.5, 3.0)
    pos_weight = gaussian(seeds[10], (D, D), HEAD ** -0.5, 0.75)
    out_weight = gaussian(seeds[11], (D, D), 8 ** -0.5, 2.0)
    up_weight = gaussian(seeds[12], (D, FF), D ** -0.5, 0.25)
    up_bias = gaussian(seeds[13], (FF,), 0.5, 3.0)
    gate_norm_gain = jnp.clip(1.0 + 0.15 * jax.random.normal(seeds[14], (HALF,), jnp.float32), 0.25, 1.75).astype(jnp.bfloat16)
    gate_norm_bias = gaussian(seeds[15], (HALF,), 0.5, 3.0)
    conv_kernel = gaussian(seeds[16], (KERNEL, HALF), KERNEL ** -0.5, 1.0)
    conv_bias = gaussian(seeds[17], (HALF,), 0.5, 3.0)
    down_weight = gaussian(seeds[18], (HALF, D), HALF ** -0.5, 0.15625)
    down_bias = gaussian(seeds[19], (D,), 0.3, 2.0)
    merge_weight = gaussian(seeds[20], (2 * D, D), (2 * D) ** -0.5, 0.1875)
    merge_bias = gaussian(seeds[21], (D,), 0.5, 3.0)
    return dict(frames=frames, lengths=lengths, cotangent=cotangent, ln_attn_gain=ln_attn_gain, ln_attn_bias=ln_attn_bias, ln_mlp_gain=ln_mlp_gain, ln_mlp_bias=ln_mlp_bias, qkv_weight=qkv_weight, content_bias=content_bias, position_bias=position_bias, pos_weight=pos_weight, out_weight=out_weight, up_weight=up_weight, up_bias=up_bias, gate_norm_gain=gate_norm_gain, gate_norm_bias=gate_norm_bias, conv_kernel=conv_kernel, conv_bias=conv_bias, down_weight=down_weight, down_bias=down_bias, merge_weight=merge_weight, merge_bias=merge_bias)


@jax.custom_vjp
def low(v):
    return lax.optimization_barrier(v.astype(jnp.bfloat16)).astype(jnp.float32)

@jax.custom_vjp
def low_back(v):
    return v

def low_keep(v):
    return (low(v), None)

def low_pass(kept, grad):
    return (grad,)

def back_keep(v):
    return (v, None)

def back_low(kept, grad):
    return (low(grad),)
low.defvjp(low_keep, low_pass)
low_back.defvjp(back_keep, back_low)
EPS = 1e-05
PRECISE = lax.Precision.HIGHEST
MASKED = -1e+30

def norm_rows(inputs, scale_row, shift_row):
    row_mean = lax.optimization_barrier(jnp.mean(inputs, axis=-1, keepdims=True))
    centred = inputs - row_mean
    spread = lax.optimization_barrier(jnp.mean(centred * centred, axis=-1, keepdims=True))
    return centred * lax.rsqrt(spread + EPS) * scale_row + shift_row

def matmul(left_side, right_side):
    return jnp.dot(left_side, right_side, precision=PRECISE, preferred_element_type=jnp.float32)

def stream_layout(lengths):
    item_ends = jnp.cumsum(lengths).astype(jnp.int32)
    first_table = jnp.concatenate([item_ends - lengths, item_ends[-1:]]).astype(jnp.int32)
    frame_index = jnp.arange(FRAMES, dtype=jnp.int32)
    item_of = lax.optimization_barrier(jnp.sum((frame_index[:, None] >= item_ends[None, :]).astype(jnp.int32), axis=1)).astype(jnp.int32)
    labels = jnp.arange(ITEMS + 1, dtype=jnp.int32)
    first_frame = lax.optimization_barrier(jnp.sum(jnp.where(item_of[:, None] == labels[None, :], first_table[None, :], 0), axis=1)).astype(jnp.int32)
    return (frame_index, item_of, frame_index - first_frame)

def angles(place_in):
    frequency = jnp.exp(jnp.arange(D // 2, dtype=jnp.float32) * (-2.0 * math.log(10000.0) / D))
    phase_angle = place_in.astype(jnp.float32)[:, None] * frequency[None, :]
    return (jnp.sin(phase_angle), jnp.cos(phase_angle))

def rel_query(projected, sine_rows, cosine_rows):
    half_size = projected.shape[-1] // 2
    first_half = projected[..., :half_size]
    second_half = projected[..., half_size:]
    sine_wide = sine_rows[:, None, :]
    cosine_wide = cosine_rows[:, None, :]
    return jnp.concatenate([first_half * sine_wide + second_half * cosine_wide, second_half * sine_wide - first_half * cosine_wide], axis=-1)

def block_layer(inputs, params, frame_index, item_of, place_in):
    ln_attn_gain, ln_attn_bias, ln_mlp_gain, ln_mlp_bias, qkv_weight, content_bias, position_bias, pos_weight, out_weight, up_weight, up_bias, gate_norm_gain, gate_norm_bias, conv_kernel, conv_bias, down_weight, down_bias, merge_weight, merge_bias = params
    row_count = inputs.shape[0]
    n_attn = low(norm_rows(inputs, ln_attn_gain, ln_attn_bias))
    n_mlp = low(norm_rows(inputs, ln_mlp_gain, ln_mlp_bias))
    qkv_rows = matmul(n_attn, qkv_weight)
    query_rows = low_back(qkv_rows[:, :D])
    key_heads = low(low_back(qkv_rows[:, D:2 * D])).reshape(row_count, HEADS, HEAD)
    value_heads = low(low_back(qkv_rows[:, 2 * D:])).reshape(row_count, HEADS, HEAD)
    q_content = low(query_rows + content_bias).reshape(row_count, HEADS, HEAD)
    q_position = low(query_rows + position_bias).reshape(row_count, HEADS, HEAD)
    projected = low_back(jnp.einsum('the,che->thc', q_position, pos_weight.reshape(D, HEADS, HEAD), precision=PRECISE))
    sine_rows, cosine_rows = angles(place_in)
    q_rel = low(rel_query(projected, sine_rows, cosine_rows))
    k_rel = low(jnp.concatenate([cosine_rows, sine_rows], axis=1))
    query_block = math.gcd(512, row_count)
    block_count = row_count // query_block

    def attend(block_args):
        content_block, rel_block, query_item, query_frame = block_args
        raw_scores = jnp.einsum('qhe,khe->hqk', content_block, key_heads, precision=PRECISE)
        raw_scores = raw_scores + jnp.einsum('qhc,kc->hqk', rel_block, k_rel, precision=PRECISE)
        raw_scores = low_back(raw_scores)
        allowed = (query_item[:, None] == item_of[None, :]) & ((query_item[:, None] < ITEMS) | (query_frame[:, None] == frame_index[None, :]))
        scaled = jnp.where(allowed[None], raw_scores * 0.125, MASKED)
        row_top = lax.optimization_barrier(jnp.max(scaled, axis=2, keepdims=True))
        weight = jnp.where(allowed[None], jnp.exp(scaled - row_top), 0.0)
        weights_low = low(weight / lax.optimization_barrier(jnp.sum(weight, axis=2, keepdims=True)))
        return jnp.einsum('hqk,khe->qhe', weights_low, value_heads, precision=PRECISE)
    mixed_heads = lax.map(jax.checkpoint(attend), (q_content.reshape(block_count, query_block, HEADS, HEAD), q_rel.reshape(block_count, query_block, HEADS, D), item_of.reshape(block_count, query_block), frame_index.reshape(block_count, query_block)))
    attn_rows = low(low_back(mixed_heads.reshape(row_count, D)))
    branch_attn = low(low_back(matmul(attn_rows, out_weight)))
    hidden_pre = low_back(matmul(n_mlp, up_weight) + up_bias)
    hidden = jax.nn.gelu(hidden_pre, approximate=False)
    gate_half = hidden[:, :HALF]
    conv_in = low(norm_rows(hidden[:, HALF:], gate_norm_gain, gate_norm_bias))
    half_width = KERNEL // 2
    padded = jnp.pad(conv_in, ((half_width, half_width), (0, 0)))
    padded_item = jnp.pad(item_of, (half_width, half_width), constant_values=-1)
    conv_out = conv_bias + jnp.zeros_like(gate_half)
    for tap_index in range(KERNEL):
        same_item = (padded_item[tap_index:tap_index + row_count] == item_of)[:, None]
        conv_out = conv_out + jnp.where(same_item, padded[tap_index:tap_index + row_count], 0.0) * conv_kernel[tap_index]
    conv_out = low_back(conv_out)
    gated_rows = low(gate_half * conv_out)
    branch_mlp = low(low_back(matmul(gated_rows, down_weight) + down_bias))
    joined = jnp.concatenate([branch_attn, branch_mlp], axis=1)
    return inputs + matmul(joined, merge_weight) + merge_bias

def reference(frames, lengths, cotangent, ln_attn_gain, ln_attn_bias, ln_mlp_gain, ln_mlp_bias, qkv_weight, content_bias, position_bias, pos_weight, out_weight, up_weight, up_bias, gate_norm_gain, gate_norm_bias, conv_kernel, conv_bias, down_weight, down_bias, merge_weight, merge_bias):
    params = tuple((weight.astype(jnp.float32) for weight in (ln_attn_gain, ln_attn_bias, ln_mlp_gain, ln_mlp_bias, qkv_weight, content_bias, position_bias, pos_weight, out_weight, up_weight, up_bias, gate_norm_gain, gate_norm_bias, conv_kernel, conv_bias, down_weight, down_bias, merge_weight, merge_bias)))

    def per_stream(totals, stream_args):
        stream_frames, stream_lengths, stream_cotangent = stream_args
        frame_index, item_of, place_in = stream_layout(stream_lengths)

        def forward(inputs, weights):
            return block_layer(inputs, weights, frame_index, item_of, place_in)
        output, pullback = jax.vjp(forward, stream_frames.astype(jnp.float32), params)
        grad_input, grad_weights = pullback(stream_cotangent.astype(jnp.float32))
        totals = jax.tree.map(jnp.add, totals, grad_weights)
        return (totals, (output.astype(jnp.bfloat16), grad_input))
    zero_grads = jax.tree.map(jnp.zeros_like, params)
    totals, stacked = lax.scan(per_stream, zero_grads, (frames, lengths, cotangent))
    return (stacked[0], stacked[1], totals[0], totals[1], totals[2], totals[3], totals[4], totals[5], totals[6], totals[7], totals[8], totals[9], totals[10], totals[11], totals[12], totals[13], totals[14], totals[15], totals[16], totals[17], totals[18])
```

```python
import math

import jax
import jax.numpy as jnp
from jax import lax
from jax.experimental import pallas as pl
from jax.experimental.pallas import tpu as pltpu
from jax.sharding import PartitionSpec as P

D = 512
HEADS = 8
HEAD = 64
KERNEL = 31
ITEMS = 5
HALF = 1536


EPS = 1e-05
MASKED = -1e30


def extended(block, sides, width):
    for axis, dim in sides:
        count = lax.axis_size(axis)
        forward = [(i, i + 1) for i in range(count - 1)]
        backward = [(target, source) for source, target in forward]
        low = lax.ppermute(
            lax.slice_in_dim(block, block.shape[dim] - width, None, axis=dim), axis, forward
        )
        high = lax.ppermute(lax.slice_in_dim(block, 0, width, axis=dim), axis, backward)
        block = jnp.concatenate([low, block, high], axis=dim)
    return block


def norm_rows(inputs, scale_row, shift_row):
    row_mean = jnp.mean(inputs, axis=-1, keepdims=True)
    centred = inputs - row_mean
    spread = jnp.mean(centred * centred, axis=-1, keepdims=True)
    return centred * lax.rsqrt(spread + EPS) * scale_row + shift_row


def gelu_exact(inputs):
    return jax.nn.gelu(inputs, approximate=False)


def frame_info(lengths, offset, extent):
    item_ends = jnp.cumsum(lengths)
    first_table = jnp.concatenate([item_ends - lengths, item_ends[-1:]])
    frame_index = offset + jnp.arange(extent, dtype=jnp.int32)
    item_of = jnp.sum((frame_index[:, None] >= item_ends[None, :]).astype(jnp.int32), axis=1)
    labels = jnp.arange(ITEMS + 1, dtype=jnp.int32)
    first_frame = jnp.sum(
        jnp.where(item_of[:, None] == labels[None, :], first_table[None, :], 0), axis=1
    )
    return (frame_index, item_of, frame_index - first_frame)


def angles(place_in):
    frequency = jnp.exp(jnp.arange(D // 2, dtype=jnp.float32) * (-2.0 * math.log(10000.0) / D))
    phase_angle = place_in.astype(jnp.float32)[:, None] * frequency[None, :]
    return (jnp.sin(phase_angle), jnp.cos(phase_angle))


def rel_query(projected, sine_rows, cosine_rows):
    half_size = projected.shape[-1] // 2
    first_half = projected[..., :half_size]
    second_half = projected[..., half_size:]
    sine_wide = sine_rows[:, None, :]
    cosine_wide = cosine_rows[:, None, :]
    return jnp.concatenate(
        [
            first_half * sine_wide + second_half * cosine_wide,
            second_half * sine_wide - first_half * cosine_wide,
        ],
        axis=-1,
    )


def step_size(extent):
    return math.gcd(extent, 512)


def score_block(q_content, q_rel, query_item, query_frame, key_block, key_start, lengths):
    extent = key_block.shape[0]
    key_frame, key_item, key_place = frame_info(lengths, key_start, extent)
    sine_rows, cosine_rows = angles(key_place)
    k_rel = jnp.concatenate([cosine_rows, sine_rows], axis=1).astype(jnp.bfloat16)
    raw_scores = jnp.einsum(
        "qhe,khe->hqk",
        q_content,
        key_block.reshape(extent, HEADS, HEAD),
        preferred_element_type=jnp.float32,
    )
    raw_scores = raw_scores + jnp.einsum(
        "qhc,kc->hqk", q_rel, k_rel, preferred_element_type=jnp.float32
    )
    allowed = (query_item[:, None] == key_item[None, :]) & (
        (query_item[:, None] < ITEMS) | (query_frame[:, None] == key_frame[None, :])
    )
    return (raw_scores, allowed, k_rel)


def block_grads(
    q_content,
    q_rel,
    query_item,
    query_frame,
    grad_out,
    log_total,
    delta_rows,
    key_block,
    value_block,
    key_start,
    lengths,
):
    extent = key_block.shape[0]
    raw_scores, allowed, k_rel = score_block(
        q_content, q_rel, query_item, query_frame, key_block, key_start, lengths
    )
    prob_rows = jnp.where(allowed[None], jnp.exp(raw_scores * 0.125 - log_total[:, :, None]), 0.0)
    grad_prob = jnp.einsum(
        "qhe,khe->hqk",
        grad_out,
        value_block.reshape(extent, HEADS, HEAD),
        preferred_element_type=jnp.float32,
    )
    grad_raw = (prob_rows * (grad_prob - delta_rows[:, :, None]) * 0.125).astype(jnp.bfloat16)
    return (prob_rows.astype(jnp.bfloat16), grad_raw, k_rel)


def frame_device(
    frames,
    lengths,
    cotangent,
    ln_attn_gain,
    ln_attn_bias,
    ln_mlp_gain,
    ln_mlp_bias,
    qkv_weight,
    content_bias,
    position_bias,
    pos_weight,
    out_weight,
    up_weight,
    up_bias,
    gate_norm_gain,
    gate_norm_bias,
    conv_kernel,
    conv_bias,
    down_weight,
    down_bias,
    merge_weight,
    merge_bias,
):
    row_count = frames.shape[1]
    cycle_size = lax.axis_size("tm")
    offset = lax.axis_index("tm") * row_count
    stream_lengths = lengths[0]
    inputs = frames[0].astype(jnp.float32)
    frame_index, item_of, place_in = frame_info(stream_lengths, offset, row_count)
    sine_rows, cosine_rows = angles(place_in)
    attn_norm, attn_pull = jax.vjp(
        norm_rows, inputs, ln_attn_gain.astype(jnp.float32), ln_attn_bias.astype(jnp.float32)
    )
    mlp_norm, mlp_pull = jax.vjp(
        norm_rows, inputs, ln_mlp_gain.astype(jnp.float32), ln_mlp_bias.astype(jnp.float32)
    )
    attn_norm_low = attn_norm.astype(jnp.bfloat16)
    mlp_norm_low = mlp_norm.astype(jnp.bfloat16)
    qkv_rows = jnp.dot(attn_norm_low, qkv_weight, preferred_element_type=jnp.float32)
    query_rows = qkv_rows[:, :D]
    key_rows = qkv_rows[:, D : 2 * D].astype(jnp.bfloat16)
    value_rows = qkv_rows[:, 2 * D :].astype(jnp.bfloat16)
    q_content = (query_rows + content_bias.astype(jnp.float32)).astype(jnp.bfloat16)
    q_position = (query_rows + position_bias.astype(jnp.float32)).astype(jnp.bfloat16)
    content_heads = q_content.reshape(row_count, HEADS, HEAD)
    position_heads = q_position.reshape(row_count, HEADS, HEAD)
    pos_heads = pos_weight.reshape(D, HEADS, HEAD)
    projected = jnp.einsum(
        "the,che->thc", position_heads, pos_heads, preferred_element_type=jnp.float32
    )
    q_rel = rel_query(projected, sine_rows, cosine_rows).astype(jnp.bfloat16)
    start_state = (
        jnp.full((HEADS, row_count), MASKED, jnp.float32),
        jnp.zeros((HEADS, row_count), jnp.float32),
        jnp.zeros((HEADS, row_count, HEAD), jnp.float32),
    )
    fold_state = start_state
    key_piece = lax.all_gather(key_rows, "tm", axis=0, tiled=True)
    value_piece = lax.all_gather(value_rows, "tm", axis=0, tiled=True)
    extent = key_piece.shape[0]
    step_rows = step_size(extent)

    def forward_one_step(inner_state, step_index):
        row_top, row_total, row_acc = inner_state
        key_block = lax.dynamic_slice_in_dim(key_piece, step_index * step_rows, step_rows, 0)
        value_block = lax.dynamic_slice_in_dim(value_piece, step_index * step_rows, step_rows, 0)
        raw_scores, allowed, k_rel = score_block(
            content_heads,
            q_rel,
            item_of,
            frame_index,
            key_block,
            step_index * step_rows,
            stream_lengths,
        )
        scaled = jnp.where(allowed[None], raw_scores * 0.125, MASKED)
        new_top = jnp.maximum(row_top, jnp.max(scaled, axis=2))
        weight = jnp.where(allowed[None], jnp.exp(scaled - new_top[:, :, None]), 0.0)
        factor = jnp.exp(row_top - new_top)
        row_total = row_total * factor + jnp.sum(weight, axis=2)
        row_acc = row_acc * factor[:, :, None] + jnp.einsum(
            "hqk,khe->hqe",
            weight.astype(jnp.bfloat16),
            value_block.reshape(step_rows, HEADS, HEAD),
            preferred_element_type=jnp.float32,
        )
        return ((new_top, row_total, row_acc), None)

    fold_state, unused = lax.scan(
        forward_one_step, fold_state, jnp.arange(extent // step_rows, dtype=jnp.int32)
    )
    row_top, row_total, row_acc = fold_state
    attn_heads = row_acc / row_total[:, :, None]
    log_total = row_top + jnp.log(row_total)
    attn_low = jnp.transpose(attn_heads, (1, 0, 2)).reshape(row_count, D).astype(jnp.bfloat16)
    branch_attn = jnp.dot(attn_low, out_weight, preferred_element_type=jnp.float32).astype(
        jnp.bfloat16
    )
    hidden_pre = jnp.dot(
        mlp_norm_low, up_weight, preferred_element_type=jnp.float32
    ) + up_bias.astype(jnp.float32)
    hidden, gelu_pull = jax.vjp(gelu_exact, hidden_pre)
    gate_half = hidden[:, :HALF]
    conv_norm, conv_pull = jax.vjp(
        norm_rows,
        hidden[:, HALF:],
        gate_norm_gain.astype(jnp.float32),
        gate_norm_bias.astype(jnp.float32),
    )
    conv_in = conv_norm.astype(jnp.bfloat16)
    half_width = KERNEL // 2
    conv_wide = extended(conv_in, (("tm", 0),), half_width)
    wide_frame, wide_item, wide_place = frame_info(
        stream_lengths, offset - half_width, row_count + 2 * half_width
    )
    kernel_rows = conv_kernel.astype(jnp.float32)
    conv_out = conv_bias.astype(jnp.float32) + jnp.zeros_like(gate_half)
    for tap_index in range(KERNEL):
        same_item = (wide_item[tap_index : tap_index + row_count] == item_of)[:, None]
        conv_out = (
            conv_out
            + jnp.where(
                same_item, conv_wide[tap_index : tap_index + row_count].astype(jnp.float32), 0.0
            )
            * kernel_rows[tap_index]
        )
    gated_low = (gate_half * conv_out).astype(jnp.bfloat16)
    branch_mlp = (
        jnp.dot(gated_low, down_weight, preferred_element_type=jnp.float32)
        + down_bias.astype(jnp.float32)
    ).astype(jnp.bfloat16)
    joined = jnp.concatenate([branch_attn, branch_mlp], axis=1)
    result = (
        inputs
        + jnp.dot(joined, merge_weight, preferred_element_type=jnp.float32)
        + merge_bias.astype(jnp.float32)
    )
    out_rows = result.astype(jnp.bfloat16)[None]
    grad_low = cotangent[0]
    grad_rows = grad_low.astype(jnp.float32)
    grad_merge_bias = jnp.sum(grad_rows, axis=0)
    grad_merge_weight = jnp.einsum(
        "tc,td->cd", joined, grad_low, preferred_element_type=jnp.float32
    )
    grad_joined = jnp.einsum(
        "td,cd->tc", grad_low, merge_weight, preferred_element_type=jnp.float32
    )
    grad_attn_branch = grad_joined[:, :D].astype(jnp.bfloat16)
    grad_mlp_branch = grad_joined[:, D:].astype(jnp.bfloat16)
    grad_down_weight = jnp.einsum(
        "tc,td->cd", gated_low, grad_mlp_branch, preferred_element_type=jnp.float32
    )
    grad_down_bias = jnp.sum(grad_mlp_branch.astype(jnp.float32), axis=0)
    grad_gated = jnp.einsum(
        "td,cd->tc", grad_mlp_branch, down_weight, preferred_element_type=jnp.float32
    )
    grad_gate_half = grad_gated * conv_out
    grad_conv_out = (grad_gated * gate_half).astype(jnp.bfloat16)
    grad_conv_rows = grad_conv_out.astype(jnp.float32)
    grad_conv_bias = jnp.sum(grad_conv_rows, axis=0)
    grad_wide = extended(grad_conv_out, (("tm", 0),), half_width)
    kernel_list = []
    grad_conv_in = jnp.zeros_like(grad_conv_rows)
    for tap_index in range(KERNEL):
        same_item = (wide_item[tap_index : tap_index + row_count] == item_of)[:, None]
        kernel_list.append(
            jnp.sum(
                jnp.where(
                    same_item, conv_wide[tap_index : tap_index + row_count].astype(jnp.float32), 0.0
                )
                * grad_conv_rows,
                axis=0,
            )
        )
        back_start = 2 * half_width - tap_index
        back_item = (wide_item[back_start : back_start + row_count] == item_of)[:, None]
        grad_conv_in = (
            grad_conv_in
            + jnp.where(
                back_item, grad_wide[back_start : back_start + row_count].astype(jnp.float32), 0.0
            )
            * kernel_rows[tap_index]
        )
    grad_conv_kernel = jnp.stack(kernel_list)
    grad_second, grad_gate_norm_gain, grad_gate_norm_bias = conv_pull(grad_conv_in)
    (grad_pre_rows,) = gelu_pull(jnp.concatenate([grad_gate_half, grad_second], axis=1))
    grad_pre = grad_pre_rows.astype(jnp.bfloat16)
    grad_up_bias = jnp.sum(grad_pre.astype(jnp.float32), axis=0)
    grad_up_weight = jnp.einsum(
        "tc,tf->cf", mlp_norm_low, grad_pre, preferred_element_type=jnp.float32
    )
    grad_mlp_norm = jnp.einsum("tf,cf->tc", grad_pre, up_weight, preferred_element_type=jnp.float32)
    grad_out_weight = jnp.einsum(
        "tc,td->cd", attn_low, grad_attn_branch, preferred_element_type=jnp.float32
    )
    grad_attn_low = jnp.einsum(
        "td,cd->tc", grad_attn_branch, out_weight, preferred_element_type=jnp.float32
    ).astype(jnp.bfloat16)
    grad_out_heads = grad_attn_low.reshape(row_count, HEADS, HEAD)
    delta_rows = jnp.sum(
        jnp.transpose(grad_out_heads.astype(jnp.float32), (1, 0, 2)) * attn_heads, axis=2
    )
    total_frames = row_count * cycle_size
    back_start_state = (
        jnp.zeros((row_count, HEADS, HEAD), jnp.float32),
        jnp.zeros((row_count, HEADS, D), jnp.float32),
        jnp.zeros((total_frames, D), jnp.float32),
        jnp.zeros((total_frames, D), jnp.float32),
    )
    back_key_piece = lax.all_gather(key_rows, "tm", axis=0, tiled=True)
    back_value_piece = lax.all_gather(value_rows, "tm", axis=0, tiled=True)
    extent = back_key_piece.shape[0]
    back_step_rows = step_size(extent)

    def back_one_step(inner_state, step_index):
        grad_content, grad_rel = inner_state
        key_block = lax.dynamic_slice_in_dim(
            back_key_piece, step_index * back_step_rows, back_step_rows, 0
        )
        value_block = lax.dynamic_slice_in_dim(
            back_value_piece, step_index * back_step_rows, back_step_rows, 0
        )
        prob_low, grad_raw, k_rel = block_grads(
            content_heads,
            q_rel,
            item_of,
            frame_index,
            grad_out_heads,
            log_total,
            delta_rows,
            key_block,
            value_block,
            step_index * back_step_rows,
            stream_lengths,
        )
        grad_content = grad_content + jnp.einsum(
            "hqk,khe->qhe",
            grad_raw,
            key_block.reshape(back_step_rows, HEADS, HEAD),
            preferred_element_type=jnp.float32,
        )
        grad_rel = grad_rel + jnp.einsum(
            "hqk,kc->qhc", grad_raw, k_rel, preferred_element_type=jnp.float32
        )
        key_part = jnp.einsum(
            "hqk,qhe->khe", grad_raw, content_heads, preferred_element_type=jnp.float32
        ).reshape(back_step_rows, D)
        value_part = jnp.einsum(
            "hqk,qhe->khe", prob_low, grad_out_heads, preferred_element_type=jnp.float32
        ).reshape(back_step_rows, D)
        return ((grad_content, grad_rel), (key_part, value_part))

    inner_state, block_parts = lax.scan(
        back_one_step,
        (back_start_state[0], back_start_state[1]),
        jnp.arange(extent // back_step_rows, dtype=jnp.int32),
    )
    key_all = block_parts[0].reshape(extent, D)
    value_all = block_parts[1].reshape(extent, D)
    grad_content, grad_rel, key_all, value_all = (
        inner_state[0],
        inner_state[1],
        key_all,
        value_all,
    )
    grad_keys, grad_values = (
        lax.psum_scatter(key_all, "tm", scatter_dimension=0, tiled=True),
        lax.psum_scatter(value_all, "tm", scatter_dimension=0, tiled=True),
    )
    half_size = D // 2
    rel_first = grad_rel[..., :half_size]
    rel_second = grad_rel[..., half_size:]
    sine_wide = sine_rows[:, None, :]
    cosine_wide = cosine_rows[:, None, :]
    grad_projected = jnp.concatenate(
        [
            rel_first * sine_wide - rel_second * cosine_wide,
            rel_first * cosine_wide + rel_second * sine_wide,
        ],
        axis=-1,
    ).astype(jnp.bfloat16)
    grad_pos_weight = jnp.einsum(
        "thc,the->che", grad_projected, position_heads, preferred_element_type=jnp.float32
    ).reshape(D, D)
    grad_q_position = jnp.einsum(
        "thc,che->the", grad_projected, pos_heads, preferred_element_type=jnp.float32
    )
    grad_content_bias = jnp.sum(grad_content, axis=0).reshape(D)
    grad_position_bias = jnp.sum(grad_q_position, axis=0).reshape(D)
    grad_query = (grad_content + grad_q_position).reshape(row_count, D).astype(jnp.bfloat16)
    grad_qkv = jnp.concatenate(
        [grad_query, grad_keys.astype(jnp.bfloat16), grad_values.astype(jnp.bfloat16)], axis=1
    )
    grad_qkv_weight = jnp.einsum(
        "tc,tf->cf", attn_norm_low, grad_qkv, preferred_element_type=jnp.float32
    )
    grad_attn_norm = jnp.einsum(
        "tf,cf->tc", grad_qkv, qkv_weight, preferred_element_type=jnp.float32
    )
    grad_from_attn, grad_ln_attn_gain, grad_ln_attn_bias = attn_pull(grad_attn_norm)
    grad_from_mlp, grad_ln_mlp_gain, grad_ln_mlp_bias = mlp_pull(grad_mlp_norm)
    grad_inputs = grad_rows + grad_from_attn + grad_from_mlp
    weight_grads = (
        grad_ln_attn_gain,
        grad_ln_attn_bias,
        grad_ln_mlp_gain,
        grad_ln_mlp_bias,
        grad_qkv_weight,
        grad_content_bias,
        grad_position_bias,
        grad_pos_weight,
        grad_out_weight,
        grad_up_weight,
        grad_up_bias,
        grad_gate_norm_gain,
        grad_gate_norm_bias,
        grad_conv_kernel,
        grad_conv_bias,
        grad_down_weight,
        grad_down_bias,
        grad_merge_weight,
        grad_merge_bias,
    )
    summed = lax.psum(
        (
            weight_grads[0],
            weight_grads[1],
            weight_grads[2],
            weight_grads[3],
            weight_grads[4],
            weight_grads[5],
            weight_grads[6],
            weight_grads[7],
            weight_grads[8],
            weight_grads[9],
            weight_grads[10],
            weight_grads[11],
            weight_grads[12],
            weight_grads[13],
            weight_grads[14],
            weight_grads[15],
            weight_grads[16],
            weight_grads[17],
            weight_grads[18],
        ),
        "tm",
    )
    shares = (
        lax.psum_scatter(
            summed[0].astype(jnp.bfloat16), "stream", scatter_dimension=0, tiled=True
        ).astype(jnp.float32),
        lax.psum_scatter(
            summed[1].astype(jnp.bfloat16), "stream", scatter_dimension=0, tiled=True
        ).astype(jnp.float32),
        lax.psum_scatter(
            summed[2].astype(jnp.bfloat16), "stream", scatter_dimension=0, tiled=True
        ).astype(jnp.float32),
        lax.psum_scatter(
            summed[3].astype(jnp.bfloat16), "stream", scatter_dimension=0, tiled=True
        ).astype(jnp.float32),
        lax.psum_scatter(
            summed[4].astype(jnp.bfloat16), "stream", scatter_dimension=0, tiled=True
        ).astype(jnp.float32),
        lax.psum_scatter(
            summed[5].astype(jnp.bfloat16), "stream", scatter_dimension=0, tiled=True
        ).astype(jnp.float32),
        lax.psum_scatter(
            summed[6].astype(jnp.bfloat16), "stream", scatter_dimension=0, tiled=True
        ).astype(jnp.float32),
        lax.psum_scatter(
            summed[7].astype(jnp.bfloat16), "stream", scatter_dimension=0, tiled=True
        ).astype(jnp.float32),
        lax.psum_scatter(
            summed[8].astype(jnp.bfloat16), "stream", scatter_dimension=0, tiled=True
        ).astype(jnp.float32),
        lax.psum_scatter(
            summed[9].astype(jnp.bfloat16), "stream", scatter_dimension=0, tiled=True
        ).astype(jnp.float32),
        lax.psum_scatter(
            summed[10].astype(jnp.bfloat16), "stream", scatter_dimension=0, tiled=True
        ).astype(jnp.float32),
        lax.psum_scatter(
            summed[11].astype(jnp.bfloat16), "stream", scatter_dimension=0, tiled=True
        ).astype(jnp.float32),
        lax.psum_scatter(
            summed[12].astype(jnp.bfloat16), "stream", scatter_dimension=0, tiled=True
        ).astype(jnp.float32),
        lax.psum_scatter(
            summed[13].astype(jnp.bfloat16), "stream", scatter_dimension=1, tiled=True
        ).astype(jnp.float32),
        lax.psum_scatter(
            summed[14].astype(jnp.bfloat16), "stream", scatter_dimension=0, tiled=True
        ).astype(jnp.float32),
        lax.psum_scatter(
            summed[15].astype(jnp.bfloat16), "stream", scatter_dimension=0, tiled=True
        ).astype(jnp.float32),
        lax.psum_scatter(
            summed[16].astype(jnp.bfloat16), "stream", scatter_dimension=0, tiled=True
        ).astype(jnp.float32),
        lax.psum_scatter(
            summed[17].astype(jnp.bfloat16), "stream", scatter_dimension=0, tiled=True
        ).astype(jnp.float32),
        lax.psum_scatter(
            summed[18].astype(jnp.bfloat16), "stream", scatter_dimension=0, tiled=True
        ).astype(jnp.float32),
    )
    return (out_rows, grad_inputs[None]) + tuple(shares)


LANES = 128
LOW = LANES // 2
BLOCK = 128
TALL = 256
WINDOW = 64
MARGIN = 16
BOUNDS = 16
VMEM_BYTES = 58 * 1024 * 1024
F32 = jnp.float32
BF16 = jnp.bfloat16


def dot_nn(left, right):
    return jnp.dot(left, right, preferred_element_type=F32)


def dot_nt(left, right):
    return lax.dot_general(left, right, (((1,), (1,)), ((), ())), preferred_element_type=F32)


def dot_tn(left, right):
    return lax.dot_general(left, right, (((0,), (0,)), ((), ())), preferred_element_type=F32)


def rows_of(index, size, base=0):
    return pl.ds(pl.multiple_of(index * size, size) + base, size)


def line_of(ref):
    return ref[...].astype(F32).reshape(1, ref.shape[0])


def fold_rows(values):
    return jnp.sum(values.reshape(values.shape[0] // 8, 8, values.shape[1]), axis=0)


def one_row(values):
    return jnp.sum(values, axis=0, keepdims=True)


def turn(values):
    return pltpu.roll(values, LOW, 1)


def low_lanes(rows):
    return lax.broadcasted_iota(jnp.int32, (rows, LANES), 1) < LOW


def centre_rows(inputs):
    mean = jnp.mean(inputs, axis=-1, keepdims=True)
    centred = inputs - mean
    spread = jnp.mean(centred * centred, axis=-1, keepdims=True)
    return centred * lax.rsqrt(spread + EPS)


ERF_SCALE = 0.3275911 / math.sqrt(2.0)
ERF_TERMS = tuple(0.5 * term for term in (1.061405429, -1.453152027, 1.421413741, -0.284496736, 0.254829592))


def gelu_parts(values):
    bell = jnp.exp(values * values * -0.5)
    size = 1.0 + ERF_SCALE * jnp.abs(values)
    place = pl.reciprocal(size, approx=True)
    place = place * (2.0 - size * place)
    series = ERF_TERMS[0]
    for term in ERF_TERMS[1:]:
        series = series * place + term
    tail = series * place * bell
    phi = jnp.where(values < 0.0, tail, 1.0 - tail)
    return values * phi, phi + values * bell * (1.0 / math.sqrt(2.0 * math.pi))


def kernel_call(body, out_shapes, in_spaces, scratch=(), flops=1 << 28, bounds=False):
    spaces = {
        "v": pl.BlockSpec(memory_space=pltpu.VMEM),
        "s": pl.BlockSpec(memory_space=pltpu.SMEM),
        "h": pl.BlockSpec((D, HALF), lambda step: (0, 1)),
    }
    scratch_shapes = [pltpu.VMEM(shape, kind) for shape, kind in scratch]
    if bounds:
        scratch_shapes.append(pltpu.SMEM((BOUNDS,), jnp.int32))
    return pl.pallas_call(
        body,
        grid=(1,) if "h" in in_spaces else (),
        out_shape=[jax.ShapeDtypeStruct(shape, kind) for shape, kind in out_shapes],
        in_specs=[spaces[space] for space in in_spaces],
        out_specs=[pl.BlockSpec(memory_space=pltpu.VMEM) for _ in out_shapes],
        scratch_shapes=scratch_shapes,
        compiler_params=pltpu.CompilerParams(vmem_limit_bytes=VMEM_BYTES),
        cost_estimate=pl.CostEstimate(flops=flops, bytes_accessed=1 << 22, transcendentals=0),
    )


def fill_bounds(lengths_ref, bounds_s, total):
    bounds_s[0] = jnp.int32(0)
    end = jnp.int32(0)
    for item in range(ITEMS):
        end = end + lengths_ref[0, item]
        bounds_s[item + 1] = end
    for item in range(ITEMS + 1, BOUNDS):
        bounds_s[item] = jnp.int32(total)


def stats_kernel(x_ref, cot_ref, gain_ref, bias_ref, up_ref, up_bias_ref, out_ref, pre_s):
    normed = centre_rows(x_ref[...].astype(F32)) * line_of(gain_ref) + line_of(bias_ref)
    pre_s[...] = dot_nn(normed.astype(BF16), up_ref[...])
    out_ref[:, :D] = cot_ref[...]
    up_bias = line_of(up_bias_ref)[:, HALF:]

    @pl.loop(0, x_ref.shape[0] // 16, unroll=2)
    def _(step):
        rows = rows_of(step, 16)
        hidden, _ = gelu_parts(pre_s[rows] + up_bias)
        mean = jnp.mean(hidden, axis=-1, keepdims=True)
        centred = hidden - mean
        rate = lax.rsqrt(jnp.mean(centred * centred, axis=-1, keepdims=True) + EPS)
        lane = lax.broadcasted_iota(jnp.int32, (16, LANES), 1)
        mean_high = mean.astype(BF16).astype(F32)
        rate_high = rate.astype(BF16).astype(F32)
        packed = jnp.where(lane == 0, mean_high, mean - mean_high)
        packed = jnp.where(lane == 2, rate_high, packed)
        packed = jnp.where(lane == 3, rate - rate_high, packed)
        out_ref[rows, D:] = packed.astype(BF16)


def select_kernel(
    up_ref,
    up_bias_ref,
    gain_ref,
    bias_ref,
    conv_bias_ref,
    taps_ref,
    qkv_ref,
    pos_ref,
    content_ref,
    position_ref,
    up_out,
    table_out,
    qkv_out,
    pos_out,
    bias_out,
):
    place = lax.axis_index("tm")
    quarters = lax.axis_size("stream")
    share = HALF // (quarters * lax.axis_size("tm"))
    lane = lax.broadcasted_iota(jnp.int32, (1, 2 * LANES), 1)
    channel = jnp.where(lane < LANES + LOW, lane, lane - LOW)
    group = jnp.zeros_like(channel)
    for quarter in range(1, quarters):
        group = group + (channel >= quarter * share).astype(jnp.int32)
    source = group * (HALF // quarters) + share * place + channel - group * share
    chosen = (lax.broadcasted_iota(jnp.int32, (HALF, 2 * LANES), 0) == source).astype(F32).astype(BF16)
    gate = dot_nn(up_ref[:, :HALF], chosen)
    conv = dot_nn(up_ref[:, HALF:], chosen)
    up_out[:, :LANES] = gate[:, :LANES].astype(BF16)
    up_out[:, LANES : 2 * LANES] = jnp.where(low_lanes(D), gate[:, LANES:], conv[:, LANES:]).astype(BF16)
    up_out[:, 2 * LANES :] = conv[:, :LANES].astype(BF16)
    up_bias = line_of(up_bias_ref)
    lines = jnp.concatenate(
        [
            up_bias[:, :HALF],
            up_bias[:, HALF:],
            line_of(gain_ref),
            line_of(bias_ref),
            line_of(conv_bias_ref),
            jnp.zeros((3, HALF), F32),
        ],
        axis=0,
    )
    lines = dot_nn(lines.astype(BF16), chosen)
    taps = dot_nn(taps_ref[...], chosen)
    for part in range(2):
        lanes = slice(part * LANES, (part + 1) * LANES)
        table_out[part, :8] = lines[:, lanes]
        table_out[part, 8 : 8 + KERNEL] = taps[:, lanes]
        table_out[part, 8 + KERNEL :] = jnp.zeros((1, LANES), F32)

    odd = lax.rem(place, 2) == 1

    def head_lanes(ref, base):
        at = pl.ds(pl.multiple_of(lax.div(place, 2) * LANES + base, LANES), LANES)
        values = ref[:, at].astype(F32)
        values = jnp.where(odd, turn(values), values)
        return jnp.where(low_lanes(values.shape[0]), values, 0.0)

    for part in range(3):
        qkv_out[:, part * LANES : (part + 1) * LANES] = head_lanes(qkv_ref, part * D).astype(BF16)
    pos_out[...] = head_lanes(pos_ref, 0).astype(BF16)
    bias_out[...] = jnp.zeros((8, LANES), F32)
    for line, ref in enumerate((content_ref, position_ref)):
        values = line_of(ref)
        picked = values[:, :LANES]
        for tile in range(1, D // LANES):
            picked = jnp.where(
                lax.div(place, 2) == tile, values[:, tile * LANES : (tile + 1) * LANES], picked
            )
        picked = jnp.where(odd, turn(picked), picked)
        bias_out[line : line + 1] = jnp.where(low_lanes(1), picked, 0.0)


def angle_rows(coarse_ref, fine_ref, block, rows):
    half = D // 2
    base = coarse_ref[pl.ds(block, 1)]
    base_sine, base_cosine = base[:, :half], base[:, half:]
    sine, cosine = fine_ref[rows, :half], fine_ref[rows, half:]
    return base_sine * cosine + base_cosine * sine, base_cosine * cosine - base_sine * sine


def item_codes(bounds_s, index):
    code = jnp.zeros_like(index)
    for item in range(1, ITEMS + 1):
        code = code + (index >= bounds_s[item]).astype(jnp.int32)
    return jnp.where(code < ITEMS, code, ITEMS + index)


def attend_kernel(
    lengths_ref,
    near_ref,
    far_ref,
    attn_gain_ref,
    attn_bias_ref,
    mlp_gain_ref,
    mlp_bias_ref,
    qkv_ref,
    pos_ref,
    bias_ref,
    coarse_ref,
    fine_ref,
    n_attn_out,
    n_mlp_out,
    hat_out,
    q_position_out,
    query_out,
    key_out,
    value_out,
    prob_out,
    attn_out,
    parts_s,
    projected_s,
    raw_s,
    bounds_s,
):
    place = lax.axis_index("tm")
    frames = n_attn_out.shape[0]
    blocks = frames // BLOCK
    half = D // 2
    fill_bounds(lengths_ref, bounds_s, frames)
    attn_gain, attn_bias = line_of(attn_gain_ref), line_of(attn_bias_ref)
    mlp_gain, mlp_bias = line_of(mlp_gain_ref), line_of(mlp_bias_ref)

    @pl.loop(0, blocks)
    def _(block):
        apart = lax.bitwise_xor(block, place)
        slot = lax.div(apart, 2)
        is_far = lax.rem(apart, 2) == 1
        for part in range(BLOCK // 32):
            at = slice(part * 32, part * 32 + 32)
            inputs = jnp.where(is_far, far_ref[slot, at].astype(F32), near_ref[slot, at].astype(F32))
            hat = centre_rows(inputs)
            rows = rows_of(block * (BLOCK // 32) + part, 32)
            hat_out[rows] = hat.astype(BF16)
            n_attn_out[rows] = (hat * attn_gain + attn_bias).astype(BF16)
            n_mlp_out[rows] = (hat * mlp_gain + mlp_bias).astype(BF16)

    @pl.loop(0, frames // TALL)
    def _(block):
        rows = rows_of(block, TALL)
        parts_s[rows] = dot_nn(n_attn_out[rows], qkv_ref[...])

    content, position = bias_ref[0:1], bias_ref[1:2]

    @pl.loop(0, frames // 64, unroll=2)
    def _(step):
        rows = rows_of(step, 64)
        query = parts_s[rows, :LANES]
        query_out[rows, :LANES] = ((query + content).astype(BF16).astype(F32) * 0.125).astype(BF16)
        q_position_out[rows] = (query + position).astype(BF16)
        key_out[rows, :LANES] = parts_s[rows, LANES : 2 * LANES].astype(BF16)
        value_out[rows] = parts_s[rows, 2 * LANES :].astype(BF16)

    @pl.loop(0, frames // TALL)
    def _(block):
        rows = rows_of(block, TALL)
        projected_s[rows] = dot_nt(q_position_out[rows], pos_ref[...])

    @pl.loop(0, blocks)
    def _(block):
        for part in range(BLOCK // 32):
            at = slice(part * 32, part * 32 + 32)
            sine, cosine = angle_rows(coarse_ref, fine_ref, block, at)
            rows = rows_of(block * (BLOCK // 32) + part, 32)
            first, second = projected_s[rows, :half], projected_s[rows, half:]
            query_out[rows, LANES : LANES + half] = ((first * sine + second * cosine) * 0.125).astype(BF16)
            query_out[rows, LANES + half :] = ((second * sine - first * cosine) * 0.125).astype(BF16)
            key_out[rows, LANES : LANES + half] = cosine.astype(BF16)
            key_out[rows, LANES + half :] = sine.astype(BF16)

    @pl.loop(0, frames // TALL)
    def _(block):
        rows = rows_of(block, TALL)
        raw_s[rows] = dot_nt(query_out[rows], key_out[...])

    key_code = item_codes(bounds_s, lax.broadcasted_iota(jnp.int32, (1, frames), 1))

    @pl.loop(0, frames // 32, unroll=2)
    def _(step):
        rows = rows_of(step, 32)
        index = step * 32 + lax.broadcasted_iota(jnp.int32, (32, 1), 0)
        scaled = jnp.where(item_codes(bounds_s, index) == key_code, raw_s[rows], MASKED)
        weight = jnp.exp(scaled - jnp.max(scaled, axis=1, keepdims=True))
        scale = 1.0 / jnp.sum(weight, axis=1, keepdims=True)
        prob_out[rows] = (weight * scale).astype(BF16)

    @pl.loop(0, frames // TALL)
    def _(block):
        rows = rows_of(block, TALL)
        attn_out[rows] = dot_nn(prob_out[rows], value_out[...])


def window_place(window, frames):
    main = frames // WINDOW
    folded = window >= main
    inner = jnp.where(folded, window - main, window)
    base = inner * WINDOW + jnp.where(folded, frames + 2 * MARGIN, 0)
    start = inner * WINDOW
    return folded.astype(jnp.int32), pl.multiple_of(base, 2 * MARGIN), start, start + jnp.where(folded, frames // 2, 0)


def item_at(bounds_s, frame):
    item = jnp.int32(0)
    for other in range(1, ITEMS + 1):
        item = item + (frame >= bounds_s[other]).astype(jnp.int32)
    return item


def over_items(bounds_s, start_low, start_high, step, init):
    first_low, first_high = item_at(bounds_s, start_low), item_at(bounds_s, start_high)
    last_low = item_at(bounds_s, start_low + WINDOW - 1)
    last_high = item_at(bounds_s, start_high + WINDOW - 1)
    low = low_lanes(8)

    def one(index, carry):
        low_item, high_item = first_low + index, first_high + index
        begin = jnp.where(low, bounds_s[low_item] - start_low, bounds_s[high_item] - start_high)
        end = jnp.where(low, bounds_s[low_item + 1] - start_low, bounds_s[high_item + 1] - start_high)
        return step(begin, end, carry)

    return lax.fori_loop(0, jnp.maximum(last_low - first_low, last_high - first_high) + 1, one, init)


def inside(begin, end, base, extent):
    shape = (extent // 8, 8, LANES)
    row = base + 8 * lax.broadcasted_iota(jnp.int32, shape, 0) + lax.broadcasted_iota(jnp.int32, shape, 1)
    return ((row >= begin[None]) & (row < end[None])).reshape(extent, LANES)


def each_tap(window):
    for shift in range(8):
        view = window[shift : shift + WINDOW + 24]
        for step in range(4):
            tap = 8 * step + shift - 1
            if 0 <= tap < KERNEL:
                yield tap, view[8 * step : 8 * step + WINDOW].reshape(WINDOW // 8, 8, LANES)


def fill_margins(wide_s, frames):
    edge = jnp.zeros((MARGIN, LANES), F32)
    wide_s[:MARGIN] = edge
    wide_s[MARGIN + frames : 2 * MARGIN + frames] = edge
    base = frames + 3 * MARGIN
    after = base + frames // 2
    low = low_lanes(MARGIN)
    wide_s[base - MARGIN : base] = jnp.where(low, 0.0, turn(wide_s[after - MARGIN : after]))
    wide_s[after : after + MARGIN] = jnp.where(low, turn(wide_s[base : base + MARGIN]), 0.0)


def mlp_first_kernel(
    lengths_ref,
    gst_ref,
    n_ref,
    up_ref,
    table_ref,
    down_ref,
    merge_ref,
    attn_ref,
    mixed_out,
    gate_pre_out,
    gy_out,
    hat_out,
    slope_out,
    down_out,
    vectors_out,
    lines_out,
    pre_s,
    hidden_s,
    gate_slope_s,
    conv_s,
    grad_s,
    out_s,
    back_s,
    branch_s,
    gated_s,
    mix_s,
    taps_s,
    turn_s,
    tap_sum_s,
    columns_s,
    down_s,
    bounds_s,
):
    place = lax.axis_index("tm")
    frames = n_ref.shape[0]
    half = frames // 2
    blocks = frames // BLOCK
    quarters, down_rows, _ = down_out.shape
    share = down_rows // 4
    channels = quarters * share
    stride = HALF // quarters
    fill_bounds(lengths_ref, bounds_s, frames)
    for part in range(2):
        for tap in range(KERNEL):
            line = jnp.broadcast_to(table_ref[part, 8 + tap : 9 + tap], (8, LANES))
            taps_s[part, tap] = line
            turn_s[part, KERNEL - 1 - tap] = line
    tap_sum_s[...] = jnp.zeros(tap_sum_s.shape, F32)
    main, rest = table_ref[0, :8], table_ref[1, :8]

    @pl.loop(0, frames // TALL)
    def _(block):
        rows = rows_of(block, TALL)
        pre_s[rows] = dot_nn(n_ref[rows], up_ref[...])

    def stat_rows(rows):
        stats = gst_ref[rows, D:].astype(F32)
        return stats[:, 0:1] + stats[:, 1:2], stats[:, 2:3] + stats[:, 3:4]

    def conv_part(hidden, mean, rate, lines, rows, to_rows):
        hat = (hidden - mean) * rate
        hat_out[rows] = hat
        conv_s[to_rows] = (hat * lines[2:3] + lines[3:4]).astype(BF16).astype(F32)

    @pl.loop(0, frames // 64)
    def _(step):
        rows = rows_of(step, 64)
        gate, gate_slope = gelu_parts(pre_s[rows, :LANES] + main[0:1])
        hidden_s[rows] = gate
        gate_slope_s[rows] = gate_slope
        hidden, slope = gelu_parts(pre_s[rows, 2 * LANES :] + main[1:2])
        slope_out[rows] = slope
        mean, rate = stat_rows(rows)
        conv_part(hidden, mean, rate, main, rows, rows_of(step, 64, MARGIN))

    @pl.loop(0, half // 64)
    def _(step):
        low = low_lanes(64)
        mixed_bias = jnp.where(low_lanes(1), rest[0:1], rest[1:2])
        low_rows, high_rows = rows_of(step, 64), rows_of(step, 64, half)
        low_hidden, low_slope = gelu_parts(pre_s[low_rows, LANES : 2 * LANES] + mixed_bias)
        high_hidden, high_slope = gelu_parts(pre_s[high_rows, LANES : 2 * LANES] + mixed_bias)
        rows = rows_of(step, 64, frames)
        hidden_s[rows] = jnp.where(low, low_hidden, turn(high_hidden))
        gate_slope_s[rows] = jnp.where(low, low_slope, turn(high_slope))
        slope_out[rows] = jnp.where(low, turn(low_slope), high_slope)
        hidden = jnp.where(low, turn(low_hidden), high_hidden)
        low_mean, low_rate = stat_rows(low_rows)
        high_mean, high_rate = stat_rows(high_rows)
        conv_part(
            hidden,
            jnp.where(low, low_mean, high_mean),
            jnp.where(low, low_rate, high_rate),
            rest,
            rows,
            rows_of(step, 64, frames + 3 * MARGIN),
        )

    fill_margins(conv_s, frames)
    windows = (frames + half) // WINDOW
    tall = WINDOW + 2 * MARGIN

    @pl.loop(0, windows)
    def _(index):
        folded, base, start_low, start_high = window_place(index, frames)
        window = conv_s[pl.ds(base, tall)]

        def step(begin, end, total):
            kept = jnp.where(inside(begin, end, -MARGIN, tall), window, 0.0)
            part = jnp.zeros((WINDOW // 8, 8, LANES), F32)
            for tap, view in each_tap(kept):
                part = part + view * taps_s[folded, tap][None]
            return jnp.where(inside(begin, end, 0, WINDOW), part.reshape(WINDOW, LANES), total)

        total = over_items(bounds_s, start_low, start_high, step, jnp.zeros((WINDOW, LANES), F32))
        out_s[rows_of(index, WINDOW)] = total + table_ref[folded, 4:5]

    for quarter in range(quarters):
        at = pl.ds(pl.multiple_of(quarter * stride + share * place, 16), share)
        down_s[quarter * share : (quarter + 1) * share] = down_ref[at]
    down_s[channels:] = jnp.zeros((2 * LANES - channels, D), BF16)

    @pl.loop(0, frames // TALL)
    def _(block):
        rows = rows_of(block, TALL)
        branch = dot_nt(gst_ref[rows, :D], merge_ref[D:]).astype(BF16)
        branch_s[rows] = branch
        gated_s[rows] = dot_nt(branch, down_s[...])

    def branch_part(grad_gated, rows, to_rows, sums):
        up_sum, conv_sum = sums
        gate, conv = hidden_s[rows], out_s[rows]
        gate_pre = (grad_gated * conv * gate_slope_s[rows]).astype(BF16)
        gate_pre_out[rows] = gate_pre
        grad_conv = (grad_gated * gate).astype(BF16).astype(F32)
        grad_s[to_rows] = grad_conv
        sums = (up_sum + fold_rows(gate_pre.astype(F32)), conv_sum + fold_rows(grad_conv))
        return gate * conv, sums

    zero = jnp.zeros((8, LANES), F32)

    def main_branch(step, sums):
        rows = rows_of(step, 64)
        gated, sums = branch_part(gated_s[rows, :LANES], rows, rows_of(step, 64, MARGIN), sums)
        mix_s[rows, :LANES] = gated.astype(BF16)
        return sums

    def rest_branch(step, sums):
        low = low_lanes(64)
        low_rows, high_rows = rows_of(step, 64), rows_of(step, 64, half)
        grad_gated = jnp.where(low, gated_s[low_rows, LANES:], turn(gated_s[high_rows, LANES:]))
        rows = rows_of(step, 64, frames)
        gated, sums = branch_part(grad_gated, rows, rows_of(step, 64, frames + 3 * MARGIN), sums)
        mix_s[low_rows, LANES:] = jnp.where(low, gated, turn(attn_ref[low_rows])).astype(BF16)
        mix_s[high_rows, LANES:] = jnp.where(low, turn(gated), turn(attn_ref[high_rows])).astype(BF16)
        return sums

    main_up, main_conv = lax.fori_loop(0, frames // 64, main_branch, (zero, zero))
    rest_up, rest_conv = lax.fori_loop(0, half // 64, rest_branch, (zero, zero))
    fill_margins(grad_s, frames)

    ones = jnp.ones((16, frames), BF16)
    lines_out[0:1] = dot_nn(ones, branch_s[...])[0:1]
    lines_out[1:2] = dot_nn(ones, gst_ref[:, :D])[0:1]
    lines_out[2:8] = jnp.zeros((6, D), F32)
    grad_down = dot_tn(mix_s[...], branch_s[...])
    for quarter in range(quarters):
        for tile in range(4):
            down_out[quarter, tile * share : (tile + 1) * share] = grad_down[
                quarter * share : (quarter + 1) * share, tile * LANES : (tile + 1) * LANES
            ].astype(BF16)

    @pl.loop(0, windows)
    def _(index):
        folded, base, start_low, start_high = window_place(index, frames)
        forward = conv_s[pl.ds(base, tall)]
        backward = grad_s[pl.ds(base, tall)]

        def step(begin, end, total):
            kept = inside(begin, end, -MARGIN, tall)
            own = jnp.where(kept, backward, 0.0)
            part = jnp.zeros((WINDOW // 8, 8, LANES), F32)
            for tap, view in each_tap(own):
                part = part + view * turn_s[folded, tap][None]
            centre = own[MARGIN : MARGIN + WINDOW].reshape(WINDOW // 8, 8, LANES)
            for tap, view in each_tap(jnp.where(kept, forward, 0.0)):
                tap_sum_s[folded, tap] += jnp.sum(view * centre, axis=0)
            return jnp.where(inside(begin, end, 0, WINDOW), part.reshape(WINDOW, LANES), total)

        back_s[rows_of(index, WINDOW)] = over_items(
            bounds_s, start_low, start_high, step, jnp.zeros((WINDOW, LANES), F32)
        )

    lane = lax.broadcasted_iota(jnp.int32, (64, LANES), 1)

    def norm_part(rows, lines, sums):
        gain_sum, bias_sum = sums
        back, hat = back_s[rows], hat_out[rows]
        grad = back * lines[2:3]
        gy_out[rows] = grad
        along = back * hat
        return grad, along * lines[2:3], (gain_sum + fold_rows(along), bias_sum + fold_rows(back))

    def two_columns(plain, along):
        plain = jnp.sum(plain, axis=-1, keepdims=True)
        along = jnp.sum(along, axis=-1, keepdims=True)
        return jnp.where(lane == 0, plain, jnp.where(lane == 1, along, 0.0))

    def main_norm(step, sums):
        rows = rows_of(step, 64)
        plain, along, sums = norm_part(rows, main, sums)
        columns_s[rows] = two_columns(plain, along)
        return sums

    def rest_norm(step, sums):
        low = low_lanes(64)
        plain, along, sums = norm_part(rows_of(step, 64, frames), rest, sums)
        columns_s[rows_of(step, 64)] += two_columns(jnp.where(low, plain, 0.0), jnp.where(low, along, 0.0))
        columns_s[rows_of(step, 64, half)] += two_columns(
            jnp.where(low, 0.0, plain), jnp.where(low, 0.0, along)
        )
        return sums

    main_gain, main_bias = lax.fori_loop(0, frames // 64, main_norm, (zero, zero))
    rest_gain, rest_bias = lax.fori_loop(0, half // 64, rest_norm, (zero, zero))

    totals = jnp.concatenate(
        [jnp.transpose(columns_s[block * BLOCK : (block + 1) * BLOCK])[:2] for block in range(blocks)], axis=0
    )
    high = totals.astype(BF16)
    low_part = (totals - high.astype(F32)).astype(BF16)
    for block in range(blocks):
        mixed_out[block, :BLOCK] = mix_s[block * BLOCK : (block + 1) * BLOCK]
        mixed_out[block, BLOCK:, :LANES] = high
        mixed_out[block, BLOCK:, LANES:] = low_part

    def vectors(part, lines):
        taps = jnp.sum(tap_sum_s[part], axis=1)[:KERNEL]
        stacked = jnp.concatenate([taps] + [one_row(line) for line in lines], axis=0)
        if part:
            stacked = stacked + turn(stacked)
        return jnp.transpose(
            jnp.concatenate([stacked, jnp.zeros((LANES - stacked.shape[0], LANES), F32)], axis=0)
        )

    vectors_out[:LANES] = vectors(0, (main_conv, main_gain, main_bias, main_up))
    vectors_out[LANES:] = vectors(1, (rest_conv, rest_gain, rest_bias, rest_up))[: channels - LANES]


def attend_back_kernel(
    gst_ref,
    n_ref,
    hat_ref,
    gain_ref,
    q_position_ref,
    query_ref,
    key_ref,
    value_ref,
    prob_ref,
    attn_ref,
    merge_ref,
    head_ref,
    pos_ref,
    qkv_ref,
    coarse_ref,
    fine_ref,
    down_ref,
    branch_out,
    total_out,
    pack_out,
    lines_out,
    grad_s,
    score_s,
    raw_s,
    query_s,
    projected_s,
    position_s,
    parts_s,
    norm_s,
):
    place = lax.axis_index("tm")
    frames = n_ref.shape[0]
    blocks = frames // BLOCK
    half = D // 2
    head = jnp.concatenate(
        [head_ref[pl.ds(pl.multiple_of(place * HEAD, HEAD), HEAD)], jnp.zeros((LANES - HEAD, D), BF16)], axis=0
    )

    @pl.loop(0, frames // TALL)
    def _(block):
        rows = rows_of(block, TALL)
        branch = dot_nt(gst_ref[rows, :D], merge_ref[:D]).astype(BF16)
        branch_out[rows] = branch
        grad = dot_nt(branch, head).astype(BF16)
        grad_s[rows] = grad
        score_s[rows] = dot_nt(grad, value_ref[...])

    @pl.loop(0, frames // 32, unroll=2)
    def _(step):
        rows = rows_of(step, 32)
        delta = jnp.sum(grad_s[rows].astype(F32) * attn_ref[rows], axis=1, keepdims=True)
        raw_s[rows] = (prob_ref[rows].astype(F32) * (score_s[rows] - delta)).astype(BF16)

    @pl.loop(0, frames // TALL)
    def _(block):
        rows = rows_of(block, TALL)
        query_s[rows] = dot_nn(raw_s[rows], key_ref[...])

    @pl.loop(0, blocks)
    def _(block):
        for part in range(BLOCK // 32):
            at = slice(part * 32, part * 32 + 32)
            sine, cosine = angle_rows(coarse_ref, fine_ref, block, at)
            rows = rows_of(block * (BLOCK // 32) + part, 32)
            first = query_s[rows, LANES : LANES + half] * 0.125
            second = query_s[rows, LANES + half :] * 0.125
            projected_s[rows, :half] = (first * sine - second * cosine).astype(BF16)
            projected_s[rows, half:] = (first * cosine + second * sine).astype(BF16)

    @pl.loop(0, frames // TALL)
    def _(block):
        rows = rows_of(block, TALL)
        position_s[rows] = dot_nn(projected_s[rows], pos_ref[...])

    zero = jnp.zeros((8, LANES), F32)

    def query_step(step, sums):
        content_sum, position_sum = sums
        rows = rows_of(step, 64)
        content, position = query_s[rows, :LANES] * 0.125, position_s[rows]
        parts_s[rows, :LANES] = (content + position).astype(BF16)
        return content_sum + fold_rows(content), position_sum + fold_rows(position)

    content_sum, position_sum = lax.fori_loop(0, frames // 64, query_step, (zero, zero))
    grad_key = dot_tn(query_ref[:, :LANES], raw_s[...])
    grad_value = dot_tn(grad_s[...], prob_ref[...])
    for block in range(blocks):
        at = slice(block * BLOCK, (block + 1) * BLOCK)
        parts_s[at, LANES : 2 * LANES] = jnp.transpose(grad_key[:, at]).astype(BF16)
        parts_s[at, 2 * LANES :] = jnp.transpose(grad_value[:, at]).astype(BF16)
    grads = [
        dot_tn(parts_s[:, :LANES], n_ref[...]),
        dot_nn(grad_key.astype(BF16), n_ref[...]),
        dot_nn(grad_value.astype(BF16), n_ref[...]),
        dot_tn(q_position_ref[...], projected_s[...]),
    ]
    for quarter in range(pack_out.shape[0]):
        lanes = slice(quarter * LANES, (quarter + 1) * LANES)
        for kind in range(4):
            pack_out[quarter, kind * HEAD : (kind + 1) * HEAD] = grads[kind][:HEAD, lanes].astype(BF16)
    spare = 4 * HEAD + down_ref.shape[1]
    pack_out[:, 4 * HEAD : spare] = down_ref[...]
    pack_out[:, spare:] = jnp.zeros((pack_out.shape[0], pack_out.shape[1] - spare, LANES), BF16)

    @pl.loop(0, frames // TALL)
    def _(block):
        rows = rows_of(block, TALL)
        norm_s[rows] = dot_nt(parts_s[rows], qkv_ref[...])

    gain = line_of(gain_ref)
    wide_zero = jnp.zeros((8, D), F32)

    def norm_step(step, sums):
        gain_sum, bias_sum = sums
        rows = rows_of(step, 32)
        grad = norm_s[rows]
        total_out[rows] = (grad * gain).astype(BF16)
        return gain_sum + fold_rows(grad * hat_ref[rows].astype(F32)), bias_sum + fold_rows(grad)

    gain_sum, bias_sum = lax.fori_loop(0, frames // 32, norm_step, (wide_zero, wide_zero))
    lane = lax.broadcasted_iota(jnp.int32, (1, LANES), 1)

    def own_lanes(sums):
        line = one_row(sums)
        line = line + turn(line)
        tiles = [
            jnp.where(lax.div(tile * LANES + lane, HEAD) == place, line, 0.0) for tile in range(D // LANES)
        ]
        return jnp.concatenate(tiles, axis=1)

    lines_out[...] = jnp.concatenate(
        [
            one_row(gain_sum),
            one_row(bias_sum),
            own_lanes(content_sum),
            own_lanes(position_sum),
            jnp.zeros((4, D), F32),
        ],
        axis=0,
    )


def mlp_second_kernel(
    gst_ref,
    mixed_ref,
    n_ref,
    norm_hat_ref,
    gain_ref,
    up_ref,
    gate_pre_ref,
    gy_ref,
    hat_ref,
    slope_ref,
    vectors_ref,
    first_lines_ref,
    head_lines_ref,
    other_ref,
    total_out,
    pack_out,
    pre_s,
    columns_s,
    norm_s,
):
    place = lax.axis_index("tm")
    frames = n_ref.shape[0]
    half = frames // 2
    blocks = frames // BLOCK
    quarters = pack_out.shape[0]
    channels = vectors_ref.shape[0]
    share = channels // quarters
    totals = jnp.zeros((2 * blocks, LANES), F32)
    for source in range(mixed_ref.shape[0]):
        both = mixed_ref[source, BLOCK:].astype(F32)
        totals = totals + (both[:, :LANES] + both[:, LANES:])
    totals = totals * (1.0 / HALF)
    columns = jnp.transpose(jnp.concatenate([totals, jnp.zeros((LANES - 2 * blocks, LANES), F32)], axis=0))
    for block in range(blocks):
        at = slice(block * BLOCK, (block + 1) * BLOCK)
        stats = gst_ref[at, D:].astype(F32)
        rate = stats[:, 2:3] + stats[:, 3:4]
        lane = lax.broadcasted_iota(jnp.int32, (BLOCK, LANES), 1)
        kept = jnp.where(lane == 0, columns[:, 2 * block : 2 * block + 1], rate)
        columns_s[at] = jnp.where(lane == 1, columns[:, 2 * block + 1 : 2 * block + 2], kept)

    def pre_part(rows, plain, along, rate, up_sum):
        grad = rate * (gy_ref[rows] - plain - hat_ref[rows] * along)
        pre = (grad * slope_ref[rows]).astype(BF16).astype(F32)
        return pre, up_sum + fold_rows(pre)

    def main_step(step, up_sum):
        rows = rows_of(step, 64)
        table = columns_s[rows]
        pre, up_sum = pre_part(rows, table[:, 0:1], table[:, 1:2], table[:, 2:3], up_sum)
        pre_s[rows, :LANES] = gate_pre_ref[rows]
        pre_s[rows, 2 * LANES :] = pre.astype(BF16)
        return up_sum

    def rest_step(step, up_sum):
        low = low_lanes(64)
        low_rows, high_rows, rows = rows_of(step, 64), rows_of(step, 64, half), rows_of(step, 64, frames)
        low_table, high_table = columns_s[low_rows], columns_s[high_rows]
        plain, along, rate = [
            jnp.where(low, low_table[:, item : item + 1], high_table[:, item : item + 1]) for item in range(3)
        ]
        pre, up_sum = pre_part(rows, plain, along, rate, up_sum)
        gate_pre = gate_pre_ref[rows].astype(F32)
        pre_s[low_rows, LANES : 2 * LANES] = jnp.where(low, gate_pre, turn(pre)).astype(BF16)
        pre_s[high_rows, LANES : 2 * LANES] = jnp.where(low, turn(gate_pre), pre).astype(BF16)
        return up_sum

    zero = jnp.zeros((8, LANES), F32)
    main_up = lax.fori_loop(0, frames // 64, main_step, zero)
    rest_up = lax.fori_loop(0, half // 64, rest_step, zero)

    @pl.loop(0, frames // TALL)
    def _(block):
        rows = rows_of(block, TALL)
        norm_s[rows] = dot_nt(pre_s[rows], up_ref[...])

    gain = line_of(gain_ref)
    wide_zero = jnp.zeros((8, D), F32)
    inner = total_out.shape[1] // 32

    def norm_step(step, sums):
        gain_sum, bias_sum = sums
        rows = rows_of(step, 32)
        grad = norm_s[rows]
        total_out[lax.div(step, inner), rows_of(lax.rem(step, inner), 32)] = (
            grad * gain + other_ref[rows].astype(F32)
        ).astype(BF16)
        return gain_sum + fold_rows(grad * norm_hat_ref[rows].astype(F32)), bias_sum + fold_rows(grad)

    gain_sum, bias_sum = lax.fori_loop(0, frames // 32, norm_step, (wide_zero, wide_zero))
    grad_up = dot_tn(pre_s[...], n_ref[...])
    gain_line, bias_line = one_row(gain_sum), one_row(bias_sum)
    rest_line = one_row(rest_up)
    up_columns = jnp.concatenate(
        [
            jnp.transpose(jnp.broadcast_to(one_row(main_up), (LANES, LANES))),
            jnp.transpose(jnp.broadcast_to(rest_line + turn(rest_line), (LANES, LANES)))[:LOW],
        ],
        axis=0,
    )
    gate_at = KERNEL + 3
    lane = lax.broadcasted_iota(jnp.int32, (share, LANES), 1)
    first_device = (place == 0).astype(F32)
    for quarter in range(quarters):
        lanes = slice(quarter * LANES, (quarter + 1) * LANES)
        pack_out[quarter, :channels] = grad_up[:channels, lanes].astype(BF16)
        pack_out[quarter, channels : channels + LANES] = grad_up[2 * LANES :, lanes].astype(BF16)
        pack_out[quarter, channels + LANES : 2 * channels] = grad_up[channels : 2 * LANES, lanes].astype(BF16)
        table = vectors_ref[quarter * share : (quarter + 1) * share]
        for other in range(2):
            source = (2 * (quarter % 2) + other) * share
            if quarter // 2 == 0:
                column = vectors_ref[source : source + share, gate_at : gate_at + 1]
            else:
                column = up_columns[source : source + share, 0:1]
            table = jnp.where(lane == gate_at + other, column, table)
        pack_out[quarter, 2 * channels : 2 * channels + share] = table.astype(BF16)
        pack_out[quarter, 2 * channels + share :] = jnp.concatenate(
            [
                head_lines_ref[0:2, lanes],
                gain_line[:, lanes],
                bias_line[:, lanes],
                head_lines_ref[2:4, lanes],
                first_lines_ref[0:2, lanes] * first_device,
                jnp.zeros((8, LANES), F32),
            ],
            axis=0,
        ).astype(BF16)


def output_kernel(
    x_ref, mixed_ref, head_ref, down_ref, down_bias_ref, merge_ref, merge_bias_ref, out_ref, joined_out
):
    sources = mixed_ref.shape[0]
    rows = x_ref.shape[0]
    channels = HALF // sources
    share = channels // 4
    attn_parts = []
    branch_attn = jnp.zeros((rows, D), F32)
    branch_mlp = jnp.zeros((rows, D), F32)
    for source in range(sources):
        attn = turn(mixed_ref[source, :rows, LANES:].astype(F32))[:, :HEAD].astype(BF16)
        attn_parts.append(attn)
        branch_attn = branch_attn + dot_nn(attn, head_ref[source * HEAD : (source + 1) * HEAD])
        down = jnp.concatenate(
            [down_ref[(part * sources + source) * share : (part * sources + source + 1) * share] for part in range(4)],
            axis=0,
        )
        branch_mlp = branch_mlp + dot_nn(mixed_ref[source, :rows, :channels], down)
    joined = jnp.concatenate(
        [branch_attn.astype(BF16), (branch_mlp + line_of(down_bias_ref)).astype(BF16)], axis=1
    )
    result = x_ref[...].astype(F32) + dot_nn(joined, merge_ref[...]) + line_of(merge_bias_ref)
    out_ref[...] = result.astype(BF16)
    turned = jnp.transpose(joined.astype(F32))
    heads = jnp.transpose(jnp.concatenate(attn_parts, axis=1).astype(F32))
    merge_share = turned.shape[0] // (4 * sources)
    head_share = heads.shape[0] // (4 * sources)
    used = 4 * (merge_share + head_share)
    for target in range(sources):
        for part in range(4):
            at = (part * sources + target) * merge_share
            joined_out[target, part * merge_share : (part + 1) * merge_share] = turned[
                at : at + merge_share
            ].astype(BF16)
            at = (part * sources + target) * head_share
            to = 4 * merge_share + part * head_share
            joined_out[target, to : to + head_share] = heads[at : at + head_share].astype(BF16)
        joined_out[target, used:] = jnp.zeros((joined_out.shape[1] - used, rows), BF16)


def merge_kernel(joined_ref, gst_ref, branch_ref, pack_out):
    sources, _, rows = joined_ref.shape
    merge_rows = 2 * D // sources
    head_rows = D // sources
    grad_merge = jnp.zeros((merge_rows, D), F32)
    grad_head = jnp.zeros((head_rows, D), F32)
    for source in range(sources):
        at = slice(source * rows, (source + 1) * rows)
        grad_merge = grad_merge + dot_nn(joined_ref[source, :merge_rows], gst_ref[at, :D])
        grad_head = grad_head + dot_nn(joined_ref[source, merge_rows : merge_rows + head_rows], branch_ref[at])
    for grad, base in ((grad_merge, 0), (grad_head, merge_rows)):
        share = grad.shape[0] // 4
        for part in range(4):
            for tile in range(4):
                to = base + tile * share
                pack_out[part, to : to + share] = grad[
                    part * share : (part + 1) * share, tile * LANES : (tile + 1) * LANES
                ].astype(BF16)


def frames_kernel(x_ref, cot_ref, total_ref, out_ref):
    for part in range(x_ref.shape[0] // 32):
        rows = slice(part * 32, part * 32 + 32)
        inputs = x_ref[rows].astype(F32)
        mean = jnp.mean(inputs, axis=-1, keepdims=True)
        centred = inputs - mean
        rate = lax.rsqrt(jnp.mean(centred * centred, axis=-1, keepdims=True) + EPS)
        hat = centred * rate
        grad = total_ref[0, rows].astype(F32)
        for source in range(1, total_ref.shape[0]):
            grad = grad + total_ref[source, rows].astype(F32)
        plain = jnp.mean(grad, axis=-1, keepdims=True)
        along = jnp.mean(grad * hat, axis=-1, keepdims=True)
        out_ref[rows] = cot_ref[rows].astype(F32) + rate * (grad - plain - hat * along)


def add_kernel(first_ref, second_ref, out_ref):
    split = first_ref.shape[1]
    for ref, rows in ((first_ref, slice(0, split)), (second_ref, slice(split, out_ref.shape[0]))):
        total = ref[0].astype(F32)
        for source in range(1, ref.shape[0]):
            total = total + ref[source].astype(F32)
        out_ref[rows] = total.astype(BF16)


def early_kernel(all_ref, qkv_out, pos_out, down_out):
    sources = all_ref.shape[0]
    share = HALF // (4 * sources)
    for kind in range(4):
        lines = jnp.transpose(
            jnp.concatenate(
                [all_ref[source, kind * HEAD : (kind + 1) * HEAD] for source in range(sources)], axis=0
            ).astype(F32)
        )
        if kind < 3:
            qkv_out[:, kind * D : (kind + 1) * D] = lines
        else:
            pos_out[...] = lines
    for source in range(sources):
        for tile in range(4):
            at = 4 * HEAD + tile * share
            down_out[source * share : (source + 1) * share, tile * LANES : (tile + 1) * LANES] = all_ref[
                source, at : at + share
            ].astype(F32)


def late_kernel(
    near_ref,
    far_ref,
    attn_gain_out,
    attn_bias_out,
    mlp_gain_out,
    mlp_bias_out,
    content_out,
    position_out,
    outw_out,
    up_out,
    up_bias_out,
    gain_out,
    bias_out,
    taps_out,
    conv_bias_out,
    down_bias_out,
    merge_out,
    merge_bias_out,
    all_s,
):
    place = lax.axis_index("tm")
    sources = all_s.shape[0]
    for source in range(sources):
        apart = lax.bitwise_xor(jnp.int32(source), place)
        slot = lax.div(apart, 2)

        @pl.when(lax.rem(apart, 2) == 0)
        def _(source=source, slot=slot):
            all_s[source] = near_ref[slot]

        @pl.when(lax.rem(apart, 2) == 1)
        def _(source=source, slot=slot):
            all_s[source] = far_ref[slot]

    channels = HALF // sources
    share = channels // 4

    def lines_at(base, size):
        return jnp.concatenate([all_s[source, base : base + size] for source in range(sources)], axis=0).astype(F32)

    for half in range(2):
        for group in range(4):
            at = half * HALF + group * sources * share
            up_out[:, at : at + sources * share] = jnp.transpose(
                lines_at(half * channels + group * share, share)
            )
    table = jnp.transpose(lines_at(2 * channels, share))
    taps_out[...] = table[:KERNEL]
    conv_bias_out[...] = table[KERNEL]
    gain_out[...] = table[KERNEL + 1]
    bias_out[...] = table[KERNEL + 2]
    wide = sources * share
    up_bias_out[:wide] = table[KERNEL + 3]
    up_bias_out[wide:] = table[KERNEL + 4]
    base = 2 * channels + share
    lines = all_s[0, base : base + 16].astype(F32)
    for source in range(1, sources):
        lines = lines + all_s[source, base : base + 16].astype(F32)
    outs = (attn_gain_out, attn_bias_out, mlp_gain_out, mlp_bias_out, content_out, position_out, down_bias_out, merge_bias_out)
    for line, out in enumerate(outs):
        out[...] = lines[line]
    base = base + 16
    merge_share = 2 * D // (4 * sources)
    head_share = D // (4 * sources)
    for source in range(sources):
        for tile in range(4):
            lanes = slice(tile * LANES, (tile + 1) * LANES)
            at = base + tile * merge_share
            merge_out[source * merge_share : (source + 1) * merge_share, lanes] = all_s[
                source, at : at + merge_share
            ].astype(F32)
            at = base + 4 * merge_share + tile * head_share
            outw_out[source * head_share : (source + 1) * head_share, lanes] = all_s[
                source, at : at + head_share
            ].astype(F32)


def spread(block, count):
    parts = [block]
    for bits in range(2, count, 2):
        parts.append(lax.ppermute(block, "tm", [(index, index ^ bits) for index in range(count)]))
    near = jnp.stack(parts)
    return near, lax.ppermute(near, "tm", [(index, index ^ 1) for index in range(count)])


def head_device(
    frames,
    lengths,
    cotangent,
    ln_attn_gain,
    ln_attn_bias,
    ln_mlp_gain,
    ln_mlp_bias,
    qkv_weight,
    content_bias,
    position_bias,
    pos_weight,
    out_weight,
    up_weight,
    up_bias,
    gate_norm_gain,
    gate_norm_bias,
    conv_kernel,
    conv_bias,
    down_weight,
    down_bias,
    merge_weight,
    merge_bias,
):
    count = lax.axis_size("tm")
    quarters = lax.axis_size("stream")
    own = frames.shape[1]
    total = own * count
    folded = total + total // 2
    padded = folded + 4 * MARGIN
    share = HALF // (quarters * count)
    channels = HALF // count
    quarter = D // quarters
    own_frames = frames[0]
    own_cotangent = cotangent[0]

    near, far = spread(own_frames, count)
    (gst_own,) = kernel_call(stats_kernel, [((own, D + LANES), BF16)], "vvvvhv", [((own, HALF), F32)])(
        own_frames, own_cotangent, ln_mlp_gain, ln_mlp_bias, up_weight, up_bias
    )
    gst = lax.all_gather(gst_own, "tm", axis=0, tiled=True)
    up_own, table, qkv_own, pos_own, bias_own = kernel_call(
        select_kernel,
        [
            ((D, 3 * LANES), BF16),
            ((2, 8 + KERNEL + 1, LANES), F32),
            ((D, 3 * LANES), BF16),
            ((D, LANES), BF16),
            ((8, LANES), F32),
        ],
        10 * "v",
    )(
        up_weight,
        up_bias,
        gate_norm_gain,
        gate_norm_bias,
        conv_bias,
        conv_kernel,
        qkv_weight,
        pos_weight,
        content_bias,
        position_bias,
    )
    frequency = jnp.exp(jnp.arange(D // 2, dtype=F32) * (-2.0 * math.log(10000.0) / D))
    coarse = jnp.arange(0, total, BLOCK, dtype=F32)[:, None] * frequency[None]
    fine = jnp.arange(BLOCK, dtype=F32)[:, None] * frequency[None]
    coarse_table = jnp.concatenate([jnp.sin(coarse), jnp.cos(coarse)], axis=1)
    fine_table = jnp.concatenate([jnp.sin(fine), jnp.cos(fine)], axis=1)

    n_attn, n_mlp, hat, q_position, query, key, value, prob, attn = kernel_call(
        attend_kernel,
        [
            ((total, D), BF16),
            ((total, D), BF16),
            ((total, D), BF16),
            ((total, LANES), BF16),
            ((total, LANES + D), BF16),
            ((total, LANES + D), BF16),
            ((total, LANES), BF16),
            ((total, total), BF16),
            ((total, LANES), F32),
        ],
        "s" + 11 * "v",
        [((total, 3 * LANES), F32), ((total, D), F32), ((total, total), F32)],
        bounds=True,
    )(
        lengths,
        near,
        far,
        ln_attn_gain,
        ln_attn_bias,
        ln_mlp_gain,
        ln_mlp_bias,
        qkv_own,
        pos_own,
        bias_own,
        coarse_table,
        fine_table,
    )

    mixed, gate_pre, grad_y, gate_hat, slope, down_pack, vectors, first_lines = kernel_call(
        mlp_first_kernel,
        [
            ((count, own + 16, 2 * LANES), BF16),
            ((folded, LANES), BF16),
            ((folded, LANES), F32),
            ((folded, LANES), F32),
            ((folded, LANES), F32),
            ((quarters, 4 * share, LANES), BF16),
            ((channels, LANES), F32),
            ((8, D), F32),
        ],
        "s" + 7 * "v",
        [
            ((total, 3 * LANES), F32),
            ((folded, LANES), F32),
            ((folded, LANES), F32),
            ((padded, LANES), F32),
            ((padded, LANES), F32),
            ((folded, LANES), F32),
            ((folded, LANES), F32),
            ((total, D), BF16),
            ((total, 2 * LANES), F32),
            ((total, 2 * LANES), BF16),
            ((2, 32, 8, LANES), F32),
            ((2, 32, 8, LANES), F32),
            ((2, 32, 8, LANES), F32),
            ((total, LANES), F32),
            ((2 * LANES, D), BF16),
        ],
        bounds=True,
    )(lengths, gst, n_mlp, up_own, table, down_weight, merge_weight, attn)
    mixed_own = lax.all_to_all(mixed, "tm", 0, 0, tiled=True)

    branch, from_attn, head_pack, head_lines = kernel_call(
        attend_back_kernel,
        [
            ((total, D), BF16),
            ((total, D), BF16),
            ((quarters, 512, LANES), BF16),
            ((8, D), F32),
        ],
        17 * "v",
        [
            ((total, LANES), BF16),
            ((total, total), F32),
            ((total, total), BF16),
            ((total, LANES + D), F32),
            ((total, D), BF16),
            ((total, LANES), F32),
            ((total, 3 * LANES), BF16),
            ((total, D), F32),
        ],
    )(
        gst,
        n_attn,
        hat,
        ln_attn_gain,
        q_position,
        query,
        key,
        value,
        prob,
        attn,
        merge_weight,
        out_weight,
        pos_own,
        qkv_own,
        coarse_table,
        fine_table,
        down_pack,
    )
    head_part = lax.psum_scatter(head_pack, "stream", scatter_dimension=0)
    head_all = lax.all_gather(head_part, "tm", axis=0)

    out_rows, joined = kernel_call(
        output_kernel,
        [((own, D), BF16), ((count, 256, own), BF16)],
        "vvvvvvv",
    )(own_frames, mixed_own, out_weight, down_weight, down_bias, merge_weight, merge_bias)
    joined_all = lax.all_to_all(joined, "tm", 0, 0, tiled=True)

    from_both, up_pack = kernel_call(
        mlp_second_kernel,
        [((count, own, D), BF16), ((quarters, 9 * share + 16, LANES), BF16)],
        14 * "v",
        [((total, 3 * LANES), BF16), ((total, LANES), F32), ((total, D), F32)],
    )(
        gst,
        mixed_own,
        n_mlp,
        hat,
        ln_mlp_gain,
        up_own,
        gate_pre,
        grad_y,
        gate_hat,
        slope,
        vectors,
        first_lines,
        head_lines,
        from_attn,
    )
    from_all = lax.all_to_all(from_both, "tm", 0, 0, tiled=True)
    up_parts = lax.all_to_all(up_pack, "stream", 0, 0, tiled=True)
    (merge_pack,) = kernel_call(
        merge_kernel, [((quarters, 4 * (3 * D // count) // quarters, LANES), BF16)], "vvv"
    )(joined_all, gst, branch)
    merge_parts = lax.all_to_all(merge_pack, "stream", 0, 0, tiled=True)
    (late_part,) = kernel_call(
        add_kernel, [((up_pack.shape[1] + merge_pack.shape[1], LANES), BF16)], "vv"
    )(up_parts, merge_parts)
    late_near, late_far = spread(late_part, count)
    (grad_frames,) = kernel_call(frames_kernel, [((own, D), F32)], "vvv")(
        own_frames, own_cotangent, from_all
    )
    grad_qkv, grad_pos, grad_down = kernel_call(
        early_kernel,
        [((quarter, 3 * D), F32), ((quarter, D), F32), ((HALF // quarters, D), F32)],
        "v",
    )(head_all)
    late = kernel_call(
        late_kernel,
        [((quarter,), F32)] * 6
        + [
            ((quarter, D), F32),
            ((quarter, 2 * HALF), F32),
            ((2 * HALF // quarters,), F32),
            ((HALF // quarters,), F32),
            ((HALF // quarters,), F32),
            ((KERNEL, HALF // quarters), F32),
            ((HALF // quarters,), F32),
            ((quarter,), F32),
            ((2 * D // quarters, D), F32),
            ((quarter,), F32),
        ],
        "vv",
        [((count,) + late_part.shape, BF16)],
    )(late_near, late_far)
    return (
        (out_rows[None], grad_frames[None])
        + tuple(late[:4])
        + (grad_qkv,)
        + tuple(late[4:6])
        + (grad_pos,)
        + tuple(late[6:13])
        + (grad_down,)
        + tuple(late[13:])
    )


def per_device(*operands):
    fits = (
        lax.axis_size("tm") == HEADS
        and lax.axis_size("stream") * LANES == D
        and operands[0].shape[1] == BLOCK
    )
    return head_device(*operands) if fits else frame_device(*operands)


def solution(mesh):
    return jax.shard_map(
        per_device,
        mesh=mesh,
        in_specs=(
            P("stream", "tm", None),
            P("stream", None),
            P("stream", "tm", None),
            P(),
            P(),
            P(),
            P(),
            P(),
            P(),
            P(),
            P(),
            P(),
            P(),
            P(),
            P(),
            P(),
            P(),
            P(),
            P(),
            P(),
            P(),
            P(),
        ),
        out_specs=(
            P("stream", "tm", None),
            P("stream", "tm", None),
            P("stream"),
            P("stream"),
            P("stream"),
            P("stream"),
            P("stream", None),
            P("stream"),
            P("stream"),
            P("stream", None),
            P("stream", None),
            P("stream", None),
            P("stream"),
            P("stream"),
            P("stream"),
            P(None, "stream"),
            P("stream"),
            P("stream", None),
            P("stream"),
            P("stream", None),
            P("stream"),
        ),
        check_vma=False,
    )
```

```python
import math

import jax
import jax.numpy as jnp
from jax import lax
from jax.experimental import pallas as pl
from jax.experimental.pallas import tpu as pltpu
from jax.sharding import PartitionSpec as P

D = 512
HEADS = 8
HEAD = 64
KERNEL = 31
ITEMS = 5
HALF = 1536


EPS = 1e-05
MASKED = -1e30


def extended(block, sides, width):
    for axis, dim in sides:
        count = lax.axis_size(axis)
        forward = [(i, i + 1) for i in range(count - 1)]
        backward = [(target, source) for source, target in forward]
        low = lax.ppermute(
            lax.slice_in_dim(block, block.shape[dim] - width, None, axis=dim), axis, forward
        )
        high = lax.ppermute(lax.slice_in_dim(block, 0, width, axis=dim), axis, backward)
        block = jnp.concatenate([low, block, high], axis=dim)
    return block


def norm_rows(inputs, scale_row, shift_row):
    row_mean = jnp.mean(inputs, axis=-1, keepdims=True)
    centred = inputs - row_mean
    spread = jnp.mean(centred * centred, axis=-1, keepdims=True)
    return centred * lax.rsqrt(spread + EPS) * scale_row + shift_row


def gelu_exact(inputs):
    return jax.nn.gelu(inputs, approximate=False)


def frame_info(lengths, offset, extent):
    item_ends = jnp.cumsum(lengths)
    first_table = jnp.concatenate([item_ends - lengths, item_ends[-1:]])
    frame_index = offset + jnp.arange(extent, dtype=jnp.int32)
    item_of = jnp.sum((frame_index[:, None] >= item_ends[None, :]).astype(jnp.int32), axis=1)
    labels = jnp.arange(ITEMS + 1, dtype=jnp.int32)
    first_frame = jnp.sum(
        jnp.where(item_of[:, None] == labels[None, :], first_table[None, :], 0), axis=1
    )
    return (frame_index, item_of, frame_index - first_frame)


def angles(place_in):
    frequency = jnp.exp(jnp.arange(D // 2, dtype=jnp.float32) * (-2.0 * math.log(10000.0) / D))
    phase_angle = place_in.astype(jnp.float32)[:, None] * frequency[None, :]
    return (jnp.sin(phase_angle), jnp.cos(phase_angle))


def rel_query(projected, sine_rows, cosine_rows):
    half_size = projected.shape[-1] // 2
    first_half = projected[..., :half_size]
    second_half = projected[..., half_size:]
    sine_wide = sine_rows[:, None, :]
    cosine_wide = cosine_rows[:, None, :]
    return jnp.concatenate(
        [
            first_half * sine_wide + second_half * cosine_wide,
            second_half * sine_wide - first_half * cosine_wide,
        ],
        axis=-1,
    )


def step_size(extent):
    return math.gcd(extent, 512)


def score_block(q_content, q_rel, query_item, query_frame, key_block, key_start, lengths):
    extent = key_block.shape[0]
    key_frame, key_item, key_place = frame_info(lengths, key_start, extent)
    sine_rows, cosine_rows = angles(key_place)
    k_rel = jnp.concatenate([cosine_rows, sine_rows], axis=1).astype(jnp.bfloat16)
    raw_scores = jnp.einsum(
        "qhe,khe->hqk",
        q_content,
        key_block.reshape(extent, HEADS, HEAD),
        preferred_element_type=jnp.float32,
    )
    raw_scores = raw_scores + jnp.einsum(
        "qhc,kc->hqk", q_rel, k_rel, preferred_element_type=jnp.float32
    )
    allowed = (query_item[:, None] == key_item[None, :]) & (
        (query_item[:, None] < ITEMS) | (query_frame[:, None] == key_frame[None, :])
    )
    return (raw_scores, allowed, k_rel)


def block_grads(
    q_content,
    q_rel,
    query_item,
    query_frame,
    grad_out,
    log_total,
    delta_rows,
    key_block,
    value_block,
    key_start,
    lengths,
):
    extent = key_block.shape[0]
    raw_scores, allowed, k_rel = score_block(
        q_content, q_rel, query_item, query_frame, key_block, key_start, lengths
    )
    prob_rows = jnp.where(allowed[None], jnp.exp(raw_scores * 0.125 - log_total[:, :, None]), 0.0)
    grad_prob = jnp.einsum(
        "qhe,khe->hqk",
        grad_out,
        value_block.reshape(extent, HEADS, HEAD),
        preferred_element_type=jnp.float32,
    )
    grad_raw = (prob_rows * (grad_prob - delta_rows[:, :, None]) * 0.125).astype(jnp.bfloat16)
    return (prob_rows.astype(jnp.bfloat16), grad_raw, k_rel)


def frame_device(
    frames,
    lengths,
    cotangent,
    ln_attn_gain,
    ln_attn_bias,
    ln_mlp_gain,
    ln_mlp_bias,
    qkv_weight,
    content_bias,
    position_bias,
    pos_weight,
    out_weight,
    up_weight,
    up_bias,
    gate_norm_gain,
    gate_norm_bias,
    conv_kernel,
    conv_bias,
    down_weight,
    down_bias,
    merge_weight,
    merge_bias,
):
    row_count = frames.shape[1]
    cycle_size = lax.axis_size("tm")
    offset = lax.axis_index("tm") * row_count
    stream_lengths = lengths[0]
    inputs = frames[0].astype(jnp.float32)
    frame_index, item_of, place_in = frame_info(stream_lengths, offset, row_count)
    sine_rows, cosine_rows = angles(place_in)
    attn_norm, attn_pull = jax.vjp(
        norm_rows, inputs, ln_attn_gain.astype(jnp.float32), ln_attn_bias.astype(jnp.float32)
    )
    mlp_norm, mlp_pull = jax.vjp(
        norm_rows, inputs, ln_mlp_gain.astype(jnp.float32), ln_mlp_bias.astype(jnp.float32)
    )
    attn_norm_low = attn_norm.astype(jnp.bfloat16)
    mlp_norm_low = mlp_norm.astype(jnp.bfloat16)
    qkv_rows = jnp.dot(attn_norm_low, qkv_weight, preferred_element_type=jnp.float32)
    query_rows = qkv_rows[:, :D]
    key_rows = qkv_rows[:, D : 2 * D].astype(jnp.bfloat16)
    value_rows = qkv_rows[:, 2 * D :].astype(jnp.bfloat16)
    q_content = (query_rows + content_bias.astype(jnp.float32)).astype(jnp.bfloat16)
    q_position = (query_rows + position_bias.astype(jnp.float32)).astype(jnp.bfloat16)
    content_heads = q_content.reshape(row_count, HEADS, HEAD)
    position_heads = q_position.reshape(row_count, HEADS, HEAD)
    pos_heads = pos_weight.reshape(D, HEADS, HEAD)
    projected = jnp.einsum(
        "the,che->thc", position_heads, pos_heads, preferred_element_type=jnp.float32
    )
    q_rel = rel_query(projected, sine_rows, cosine_rows).astype(jnp.bfloat16)
    start_state = (
        jnp.full((HEADS, row_count), MASKED, jnp.float32),
        jnp.zeros((HEADS, row_count), jnp.float32),
        jnp.zeros((HEADS, row_count, HEAD), jnp.float32),
    )
    fold_state = start_state
    key_piece = lax.all_gather(key_rows, "tm", axis=0, tiled=True)
    value_piece = lax.all_gather(value_rows, "tm", axis=0, tiled=True)
    extent = key_piece.shape[0]
    step_rows = step_size(extent)

    def forward_one_step(inner_state, step_index):
        row_top, row_total, row_acc = inner_state
        key_block = lax.dynamic_slice_in_dim(key_piece, step_index * step_rows, step_rows, 0)
        value_block = lax.dynamic_slice_in_dim(value_piece, step_index * step_rows, step_rows, 0)
        raw_scores, allowed, k_rel = score_block(
            content_heads,
            q_rel,
            item_of,
            frame_index,
            key_block,
            step_index * step_rows,
            stream_lengths,
        )
        scaled = jnp.where(allowed[None], raw_scores * 0.125, MASKED)
        new_top = jnp.maximum(row_top, jnp.max(scaled, axis=2))
        weight = jnp.where(allowed[None], jnp.exp(scaled - new_top[:, :, None]), 0.0)
        factor = jnp.exp(row_top - new_top)
        row_total = row_total * factor + jnp.sum(weight, axis=2)
        row_acc = row_acc * factor[:, :, None] + jnp.einsum(
            "hqk,khe->hqe",
            weight.astype(jnp.bfloat16),
            value_block.reshape(step_rows, HEADS, HEAD),
            preferred_element_type=jnp.float32,
        )
        return ((new_top, row_total, row_acc), None)

    fold_state, unused = lax.scan(
        forward_one_step, fold_state, jnp.arange(extent // step_rows, dtype=jnp.int32)
    )
    row_top, row_total, row_acc = fold_state
    attn_heads = row_acc / row_total[:, :, None]
    log_total = row_top + jnp.log(row_total)
    attn_low = jnp.transpose(attn_heads, (1, 0, 2)).reshape(row_count, D).astype(jnp.bfloat16)
    branch_attn = jnp.dot(attn_low, out_weight, preferred_element_type=jnp.float32).astype(
        jnp.bfloat16
    )
    hidden_pre = jnp.dot(
        mlp_norm_low, up_weight, preferred_element_type=jnp.float32
    ) + up_bias.astype(jnp.float32)
    hidden, gelu_pull = jax.vjp(gelu_exact, hidden_pre)
    gate_half = hidden[:, :HALF]
    conv_norm, conv_pull = jax.vjp(
        norm_rows,
        hidden[:, HALF:],
        gate_norm_gain.astype(jnp.float32),
        gate_norm_bias.astype(jnp.float32),
    )
    conv_in = conv_norm.astype(jnp.bfloat16)
    half_width = KERNEL // 2
    conv_wide = extended(conv_in, (("tm", 0),), half_width)
    wide_frame, wide_item, wide_place = frame_info(
        stream_lengths, offset - half_width, row_count + 2 * half_width
    )
    kernel_rows = conv_kernel.astype(jnp.float32)
    conv_out = conv_bias.astype(jnp.float32) + jnp.zeros_like(gate_half)
    for tap_index in range(KERNEL):
        same_item = (wide_item[tap_index : tap_index + row_count] == item_of)[:, None]
        conv_out = (
            conv_out
            + jnp.where(
                same_item, conv_wide[tap_index : tap_index + row_count].astype(jnp.float32), 0.0
            )
            * kernel_rows[tap_index]
        )
    gated_low = (gate_half * conv_out).astype(jnp.bfloat16)
    branch_mlp = (
        jnp.dot(gated_low, down_weight, preferred_element_type=jnp.float32)
        + down_bias.astype(jnp.float32)
    ).astype(jnp.bfloat16)
    joined = jnp.concatenate([branch_attn, branch_mlp], axis=1)
    result = (
        inputs
        + jnp.dot(joined, merge_weight, preferred_element_type=jnp.float32)
        + merge_bias.astype(jnp.float32)
    )
    out_rows = result.astype(jnp.bfloat16)[None]
    grad_low = cotangent[0]
    grad_rows = grad_low.astype(jnp.float32)
    grad_merge_bias = jnp.sum(grad_rows, axis=0)
    grad_merge_weight = jnp.einsum(
        "tc,td->cd", joined, grad_low, preferred_element_type=jnp.float32
    )
    grad_joined = jnp.einsum(
        "td,cd->tc", grad_low, merge_weight, preferred_element_type=jnp.float32
    )
    grad_attn_branch = grad_joined[:, :D].astype(jnp.bfloat16)
    grad_mlp_branch = grad_joined[:, D:].astype(jnp.bfloat16)
    grad_down_weight = jnp.einsum(
        "tc,td->cd", gated_low, grad_mlp_branch, preferred_element_type=jnp.float32
    )
    grad_down_bias = jnp.sum(grad_mlp_branch.astype(jnp.float32), axis=0)
    grad_gated = jnp.einsum(
        "td,cd->tc", grad_mlp_branch, down_weight, preferred_element_type=jnp.float32
    )
    grad_gate_half = grad_gated * conv_out
    grad_conv_out = (grad_gated * gate_half).astype(jnp.bfloat16)
    grad_conv_rows = grad_conv_out.astype(jnp.float32)
    grad_conv_bias = jnp.sum(grad_conv_rows, axis=0)
    grad_wide = extended(grad_conv_out, (("tm", 0),), half_width)
    kernel_list = []
    grad_conv_in = jnp.zeros_like(grad_conv_rows)
    for tap_index in range(KERNEL):
        same_item = (wide_item[tap_index : tap_index + row_count] == item_of)[:, None]
        kernel_list.append(
            jnp.sum(
                jnp.where(
                    same_item, conv_wide[tap_index : tap_index + row_count].astype(jnp.float32), 0.0
                )
                * grad_conv_rows,
                axis=0,
            )
        )
        back_start = 2 * half_width - tap_index
        back_item = (wide_item[back_start : back_start + row_count] == item_of)[:, None]
        grad_conv_in = (
            grad_conv_in
            + jnp.where(
                back_item, grad_wide[back_start : back_start + row_count].astype(jnp.float32), 0.0
            )
            * kernel_rows[tap_index]
        )
    grad_conv_kernel = jnp.stack(kernel_list)
    grad_second, grad_gate_norm_gain, grad_gate_norm_bias = conv_pull(grad_conv_in)
    (grad_pre_rows,) = gelu_pull(jnp.concatenate([grad_gate_half, grad_second], axis=1))
    grad_pre = grad_pre_rows.astype(jnp.bfloat16)
    grad_up_bias = jnp.sum(grad_pre.astype(jnp.float32), axis=0)
    grad_up_weight = jnp.einsum(
        "tc,tf->cf", mlp_norm_low, grad_pre, preferred_element_type=jnp.float32
    )
    grad_mlp_norm = jnp.einsum("tf,cf->tc", grad_pre, up_weight, preferred_element_type=jnp.float32)
    grad_out_weight = jnp.einsum(
        "tc,td->cd", attn_low, grad_attn_branch, preferred_element_type=jnp.float32
    )
    grad_attn_low = jnp.einsum(
        "td,cd->tc", grad_attn_branch, out_weight, preferred_element_type=jnp.float32
    ).astype(jnp.bfloat16)
    grad_out_heads = grad_attn_low.reshape(row_count, HEADS, HEAD)
    delta_rows = jnp.sum(
        jnp.transpose(grad_out_heads.astype(jnp.float32), (1, 0, 2)) * attn_heads, axis=2
    )
    total_frames = row_count * cycle_size
    back_start_state = (
        jnp.zeros((row_count, HEADS, HEAD), jnp.float32),
        jnp.zeros((row_count, HEADS, D), jnp.float32),
        jnp.zeros((total_frames, D), jnp.float32),
        jnp.zeros((total_frames, D), jnp.float32),
    )
    back_key_piece = lax.all_gather(key_rows, "tm", axis=0, tiled=True)
    back_value_piece = lax.all_gather(value_rows, "tm", axis=0, tiled=True)
    extent = back_key_piece.shape[0]
    back_step_rows = step_size(extent)

    def back_one_step(inner_state, step_index):
        grad_content, grad_rel = inner_state
        key_block = lax.dynamic_slice_in_dim(
            back_key_piece, step_index * back_step_rows, back_step_rows, 0
        )
        value_block = lax.dynamic_slice_in_dim(
            back_value_piece, step_index * back_step_rows, back_step_rows, 0
        )
        prob_low, grad_raw, k_rel = block_grads(
            content_heads,
            q_rel,
            item_of,
            frame_index,
            grad_out_heads,
            log_total,
            delta_rows,
            key_block,
            value_block,
            step_index * back_step_rows,
            stream_lengths,
        )
        grad_content = grad_content + jnp.einsum(
            "hqk,khe->qhe",
            grad_raw,
            key_block.reshape(back_step_rows, HEADS, HEAD),
            preferred_element_type=jnp.float32,
        )
        grad_rel = grad_rel + jnp.einsum(
            "hqk,kc->qhc", grad_raw, k_rel, preferred_element_type=jnp.float32
        )
        key_part = jnp.einsum(
            "hqk,qhe->khe", grad_raw, content_heads, preferred_element_type=jnp.float32
        ).reshape(back_step_rows, D)
        value_part = jnp.einsum(
            "hqk,qhe->khe", prob_low, grad_out_heads, preferred_element_type=jnp.float32
        ).reshape(back_step_rows, D)
        return ((grad_content, grad_rel), (key_part, value_part))

    inner_state, block_parts = lax.scan(
        back_one_step,
        (back_start_state[0], back_start_state[1]),
        jnp.arange(extent // back_step_rows, dtype=jnp.int32),
    )
    key_all = block_parts[0].reshape(extent, D)
    value_all = block_parts[1].reshape(extent, D)
    grad_content, grad_rel, key_all, value_all = (
        inner_state[0],
        inner_state[1],
        key_all,
        value_all,
    )
    grad_keys, grad_values = (
        lax.psum_scatter(key_all, "tm", scatter_dimension=0, tiled=True),
        lax.psum_scatter(value_all, "tm", scatter_dimension=0, tiled=True),
    )
    half_size = D // 2
    rel_first = grad_rel[..., :half_size]
    rel_second = grad_rel[..., half_size:]
    sine_wide = sine_rows[:, None, :]
    cosine_wide = cosine_rows[:, None, :]
    grad_projected = jnp.concatenate(
        [
            rel_first * sine_wide - rel_second * cosine_wide,
            rel_first * cosine_wide + rel_second * sine_wide,
        ],
        axis=-1,
    ).astype(jnp.bfloat16)
    grad_pos_weight = jnp.einsum(
        "thc,the->che", grad_projected, position_heads, preferred_element_type=jnp.float32
    ).reshape(D, D)
    grad_q_position = jnp.einsum(
        "thc,che->the", grad_projected, pos_heads, preferred_element_type=jnp.float32
    )
    grad_content_bias = jnp.sum(grad_content, axis=0).reshape(D)
    grad_position_bias = jnp.sum(grad_q_position, axis=0).reshape(D)
    grad_query = (grad_content + grad_q_position).reshape(row_count, D).astype(jnp.bfloat16)
    grad_qkv = jnp.concatenate(
        [grad_query, grad_keys.astype(jnp.bfloat16), grad_values.astype(jnp.bfloat16)], axis=1
    )
    grad_qkv_weight = jnp.einsum(
        "tc,tf->cf", attn_norm_low, grad_qkv, preferred_element_type=jnp.float32
    )
    grad_attn_norm = jnp.einsum(
        "tf,cf->tc", grad_qkv, qkv_weight, preferred_element_type=jnp.float32
    )
    grad_from_attn, grad_ln_attn_gain, grad_ln_attn_bias = attn_pull(grad_attn_norm)
    grad_from_mlp, grad_ln_mlp_gain, grad_ln_mlp_bias = mlp_pull(grad_mlp_norm)
    grad_inputs = grad_rows + grad_from_attn + grad_from_mlp
    weight_grads = (
        grad_ln_attn_gain,
        grad_ln_attn_bias,
        grad_ln_mlp_gain,
        grad_ln_mlp_bias,
        grad_qkv_weight,
        grad_content_bias,
        grad_position_bias,
        grad_pos_weight,
        grad_out_weight,
        grad_up_weight,
        grad_up_bias,
        grad_gate_norm_gain,
        grad_gate_norm_bias,
        grad_conv_kernel,
        grad_conv_bias,
        grad_down_weight,
        grad_down_bias,
        grad_merge_weight,
        grad_merge_bias,
    )
    summed = lax.psum(
        (
            weight_grads[0],
            weight_grads[1],
            weight_grads[2],
            weight_grads[3],
            weight_grads[4],
            weight_grads[5],
            weight_grads[6],
            weight_grads[7],
            weight_grads[8],
            weight_grads[9],
            weight_grads[10],
            weight_grads[11],
            weight_grads[12],
            weight_grads[13],
            weight_grads[14],
            weight_grads[15],
            weight_grads[16],
            weight_grads[17],
            weight_grads[18],
        ),
        "tm",
    )
    shares = (
        lax.psum_scatter(
            summed[0].astype(jnp.bfloat16), "stream", scatter_dimension=0, tiled=True
        ).astype(jnp.float32),
        lax.psum_scatter(
            summed[1].astype(jnp.bfloat16), "stream", scatter_dimension=0, tiled=True
        ).astype(jnp.float32),
        lax.psum_scatter(
            summed[2].astype(jnp.bfloat16), "stream", scatter_dimension=0, tiled=True
        ).astype(jnp.float32),
        lax.psum_scatter(
            summed[3].astype(jnp.bfloat16), "stream", scatter_dimension=0, tiled=True
        ).astype(jnp.float32),
        lax.psum_scatter(
            summed[4].astype(jnp.bfloat16), "stream", scatter_dimension=0, tiled=True
        ).astype(jnp.float32),
        lax.psum_scatter(
            summed[5].astype(jnp.bfloat16), "stream", scatter_dimension=0, tiled=True
        ).astype(jnp.float32),
        lax.psum_scatter(
            summed[6].astype(jnp.bfloat16), "stream", scatter_dimension=0, tiled=True
        ).astype(jnp.float32),
        lax.psum_scatter(
            summed[7].astype(jnp.bfloat16), "stream", scatter_dimension=0, tiled=True
        ).astype(jnp.float32),
        lax.psum_scatter(
            summed[8].astype(jnp.bfloat16), "stream", scatter_dimension=0, tiled=True
        ).astype(jnp.float32),
        lax.psum_scatter(
            summed[9].astype(jnp.bfloat16), "stream", scatter_dimension=0, tiled=True
        ).astype(jnp.float32),
        lax.psum_scatter(
            summed[10].astype(jnp.bfloat16), "stream", scatter_dimension=0, tiled=True
        ).astype(jnp.float32),
        lax.psum_scatter(
            summed[11].astype(jnp.bfloat16), "stream", scatter_dimension=0, tiled=True
        ).astype(jnp.float32),
        lax.psum_scatter(
            summed[12].astype(jnp.bfloat16), "stream", scatter_dimension=0, tiled=True
        ).astype(jnp.float32),
        lax.psum_scatter(
            summed[13].astype(jnp.bfloat16), "stream", scatter_dimension=1, tiled=True
        ).astype(jnp.float32),
        lax.psum_scatter(
            summed[14].astype(jnp.bfloat16), "stream", scatter_dimension=0, tiled=True
        ).astype(jnp.float32),
        lax.psum_scatter(
            summed[15].astype(jnp.bfloat16), "stream", scatter_dimension=0, tiled=True
        ).astype(jnp.float32),
        lax.psum_scatter(
            summed[16].astype(jnp.bfloat16), "stream", scatter_dimension=0, tiled=True
        ).astype(jnp.float32),
        lax.psum_scatter(
            summed[17].astype(jnp.bfloat16), "stream", scatter_dimension=0, tiled=True
        ).astype(jnp.float32),
        lax.psum_scatter(
            summed[18].astype(jnp.bfloat16), "stream", scatter_dimension=0, tiled=True
        ).astype(jnp.float32),
    )
    return (out_rows, grad_inputs[None]) + tuple(shares)


LANES = 128
LOW = LANES // 2
BLOCK = 128
TALL = 256
WINDOW = 64
MARGIN = 16
BOUNDS = 16
MEGA = 1024 * 1024
RATE = 1150000000
F32 = jnp.float32
BF16 = jnp.bfloat16


def dot_nn(left, right):
    return jnp.dot(left, right, preferred_element_type=F32)


def dot_nt(left, right):
    return lax.dot_general(left, right, (((1,), (1,)), ((), ())), preferred_element_type=F32)


def dot_tn(left, right):
    return lax.dot_general(left, right, (((0,), (0,)), ((), ())), preferred_element_type=F32)


def rows_of(index, size, base=0):
    return pl.ds(pl.multiple_of(index * size, size) + base, size)


def line_of(ref):
    return ref[...].astype(F32).reshape(1, ref.shape[0])


def fold_rows(values):
    return jnp.sum(values.reshape(values.shape[0] // 8, 8, values.shape[1]), axis=0)


def one_row(values):
    return jnp.sum(values, axis=0, keepdims=True)


def turn(values):
    return pltpu.roll(values, LOW, 1)


def low_lanes(rows):
    return lax.broadcasted_iota(jnp.int32, (rows, LANES), 1) < LOW


def centre_rows(inputs):
    mean = jnp.mean(inputs, axis=-1, keepdims=True)
    centred = inputs - mean
    spread = jnp.mean(centred * centred, axis=-1, keepdims=True)
    return centred * lax.rsqrt(spread + EPS)


ERF_SCALE = 0.3275911 / math.sqrt(2.0)
ERF_TERMS = tuple(0.5 * term for term in (1.061405429, -1.453152027, 1.421413741, -0.284496736, 0.254829592))


def gelu_parts(values):
    bell = jnp.exp(values * values * -0.5)
    size = 1.0 + ERF_SCALE * jnp.abs(values)
    place = pl.reciprocal(size, approx=True)
    place = place * (2.0 - size * place)
    series = ERF_TERMS[0]
    for term in ERF_TERMS[1:]:
        series = series * place + term
    tail = series * place * bell
    phi = jnp.where(values < 0.0, tail, 1.0 - tail)
    return values * phi, phi + values * bell * (1.0 / math.sqrt(2.0 * math.pi))


def kernel_call(body, out_shapes, in_spaces, scratch=(), micros=2, megas=32, bounds=False):
    spaces = {
        "v": pl.BlockSpec(memory_space=pltpu.VMEM),
        "s": pl.BlockSpec(memory_space=pltpu.SMEM),
        "h": pl.BlockSpec((D, HALF), lambda step: (0, 1)),
    }
    scratch_shapes = [pltpu.VMEM(shape, kind) for shape, kind in scratch]
    if bounds:
        scratch_shapes.append(pltpu.SMEM((BOUNDS,), jnp.int32))
    return pl.pallas_call(
        body,
        grid=(1,) if "h" in in_spaces else (),
        out_shape=[jax.ShapeDtypeStruct(shape, kind) for shape, kind in out_shapes],
        in_specs=[spaces[space] for space in in_spaces],
        out_specs=[pl.BlockSpec(memory_space=pltpu.VMEM) for _ in out_shapes],
        scratch_shapes=scratch_shapes,
        compiler_params=pltpu.CompilerParams(vmem_limit_bytes=megas * MEGA),
        cost_estimate=pl.CostEstimate(flops=micros * RATE, bytes_accessed=1 << 20, transcendentals=0),
    )


def fill_bounds(lengths_ref, bounds_s, total):
    bounds_s[0] = jnp.int32(0)
    end = jnp.int32(0)
    for item in range(ITEMS):
        end = end + lengths_ref[0, item]
        bounds_s[item + 1] = end
    for item in range(ITEMS + 1, BOUNDS):
        bounds_s[item] = jnp.int32(total)


def stats_kernel(x_ref, cot_ref, gain_ref, bias_ref, up_ref, up_bias_ref, out_ref, pre_s):
    normed = centre_rows(x_ref[...].astype(F32)) * line_of(gain_ref) + line_of(bias_ref)
    pre_s[...] = dot_nn(normed.astype(BF16), up_ref[...])
    out_ref[:, :D] = cot_ref[...]
    up_bias = line_of(up_bias_ref)[:, HALF:]

    @pl.loop(0, x_ref.shape[0] // 16, unroll=2)
    def _(step):
        rows = rows_of(step, 16)
        hidden, _ = gelu_parts(pre_s[rows] + up_bias)
        mean = jnp.mean(hidden, axis=-1, keepdims=True)
        centred = hidden - mean
        rate = lax.rsqrt(jnp.mean(centred * centred, axis=-1, keepdims=True) + EPS)
        lane = lax.broadcasted_iota(jnp.int32, (16, LANES), 1)
        mean_high = mean.astype(BF16).astype(F32)
        rate_high = rate.astype(BF16).astype(F32)
        packed = jnp.where(lane == 0, mean_high, mean - mean_high)
        packed = jnp.where(lane == 2, rate_high, packed)
        packed = jnp.where(lane == 3, rate - rate_high, packed)
        out_ref[rows, D:] = packed.astype(BF16)


def select_kernel(
    up_ref,
    up_bias_ref,
    gain_ref,
    bias_ref,
    conv_bias_ref,
    taps_ref,
    qkv_ref,
    pos_ref,
    content_ref,
    position_ref,
    up_out,
    table_out,
    qkv_out,
    pos_out,
    bias_out,
):
    place = lax.axis_index("tm")
    quarters = lax.axis_size("stream")
    share = HALF // (quarters * lax.axis_size("tm"))
    lane = lax.broadcasted_iota(jnp.int32, (1, 2 * LANES), 1)
    channel = jnp.where(lane < LANES + LOW, lane, lane - LOW)
    group = jnp.zeros_like(channel)
    for quarter in range(1, quarters):
        group = group + (channel >= quarter * share).astype(jnp.int32)
    source = group * (HALF // quarters) + share * place + channel - group * share
    chosen = (lax.broadcasted_iota(jnp.int32, (HALF, 2 * LANES), 0) == source).astype(F32).astype(BF16)
    gate = dot_nn(up_ref[:, :HALF], chosen)
    conv = dot_nn(up_ref[:, HALF:], chosen)
    up_out[:, :LANES] = gate[:, :LANES].astype(BF16)
    up_out[:, LANES : 2 * LANES] = jnp.where(low_lanes(D), gate[:, LANES:], conv[:, LANES:]).astype(BF16)
    up_out[:, 2 * LANES :] = conv[:, :LANES].astype(BF16)
    up_bias = line_of(up_bias_ref)
    lines = jnp.concatenate(
        [
            up_bias[:, :HALF],
            up_bias[:, HALF:],
            line_of(gain_ref),
            line_of(bias_ref),
            line_of(conv_bias_ref),
            jnp.zeros((3, HALF), F32),
        ],
        axis=0,
    )
    lines = dot_nn(lines.astype(BF16), chosen)
    taps = dot_nn(taps_ref[...], chosen)
    for part in range(2):
        lanes = slice(part * LANES, (part + 1) * LANES)
        table_out[part, :8] = lines[:, lanes]
        table_out[part, 8 : 8 + KERNEL] = taps[:, lanes]
        table_out[part, 8 + KERNEL :] = jnp.zeros((1, LANES), F32)

    odd = lax.rem(place, 2) == 1

    def head_lanes(ref, base):
        at = pl.ds(pl.multiple_of(lax.div(place, 2) * LANES + base, LANES), LANES)
        values = ref[:, at].astype(F32)
        values = jnp.where(odd, turn(values), values)
        return jnp.where(low_lanes(values.shape[0]), values, 0.0)

    for part in range(3):
        qkv_out[:, part * LANES : (part + 1) * LANES] = head_lanes(qkv_ref, part * D).astype(BF16)
    pos_out[...] = head_lanes(pos_ref, 0).astype(BF16)
    bias_out[...] = jnp.zeros((8, LANES), F32)
    for line, ref in enumerate((content_ref, position_ref)):
        values = line_of(ref)
        picked = values[:, :LANES]
        for tile in range(1, D // LANES):
            picked = jnp.where(
                lax.div(place, 2) == tile, values[:, tile * LANES : (tile + 1) * LANES], picked
            )
        picked = jnp.where(odd, turn(picked), picked)
        bias_out[line : line + 1] = jnp.where(low_lanes(1), picked, 0.0)


def angle_rows(coarse_ref, fine_ref, block, rows):
    half = D // 2
    base = coarse_ref[pl.ds(block, 1)]
    base_sine, base_cosine = base[:, :half], base[:, half:]
    sine, cosine = fine_ref[rows, :half], fine_ref[rows, half:]
    return base_sine * cosine + base_cosine * sine, base_cosine * cosine - base_sine * sine


def item_codes(bounds_s, index):
    code = jnp.zeros_like(index)
    for item in range(1, ITEMS + 1):
        code = code + (index >= bounds_s[item]).astype(jnp.int32)
    return jnp.where(code < ITEMS, code, ITEMS + index)


def attend_kernel(lengths_ref, *refs):
    x_refs = refs[:HEADS]
    (
        attn_gain_ref,
        attn_bias_ref,
        mlp_gain_ref,
        mlp_bias_ref,
        qkv_ref,
        pos_ref,
        bias_ref,
        coarse_ref,
        fine_ref,
        n_attn_out,
        n_mlp_out,
        hat_out,
        q_position_out,
        query_out,
        key_out,
        value_out,
        prob_out,
        attn_out,
        share_out,
        parts_s,
        projected_s,
        raw_s,
        bounds_s,
    ) = refs[HEADS:]
    place = lax.axis_index("tm")
    frames = n_attn_out.shape[0]
    blocks = frames // BLOCK
    half = D // 2
    fill_bounds(lengths_ref, bounds_s, frames)
    attn_gain, attn_bias = line_of(attn_gain_ref), line_of(attn_bias_ref)
    mlp_gain, mlp_bias = line_of(mlp_gain_ref), line_of(mlp_bias_ref)

    for apart, x_ref in enumerate(x_refs):
        block = lax.bitwise_xor(jnp.int32(apart), place)
        for part in range(BLOCK // 32):
            hat = centre_rows(x_ref[part * 32 : part * 32 + 32].astype(F32))
            rows = rows_of(block * (BLOCK // 32) + part, 32)
            hat_out[rows] = hat.astype(BF16)
            n_attn_out[rows] = (hat * attn_gain + attn_bias).astype(BF16)
            n_mlp_out[rows] = (hat * mlp_gain + mlp_bias).astype(BF16)

    @pl.loop(0, frames // TALL)
    def _(block):
        rows = rows_of(block, TALL)
        parts_s[rows] = dot_nn(n_attn_out[rows], qkv_ref[...])

    content, position = bias_ref[0:1], bias_ref[1:2]

    @pl.loop(0, frames // 64, unroll=2)
    def _(step):
        rows = rows_of(step, 64)
        query = parts_s[rows, :LANES]
        query_out[rows, :LANES] = ((query + content).astype(BF16).astype(F32) * 0.125).astype(BF16)
        q_position_out[rows] = (query + position).astype(BF16)
        key_out[rows, :LANES] = parts_s[rows, LANES : 2 * LANES].astype(BF16)
        value_out[rows] = parts_s[rows, 2 * LANES :].astype(BF16)

    @pl.loop(0, frames // TALL)
    def _(block):
        rows = rows_of(block, TALL)
        projected_s[rows] = dot_nt(q_position_out[rows], pos_ref[...])

    @pl.loop(0, blocks)
    def _(block):
        for part in range(BLOCK // 32):
            at = slice(part * 32, part * 32 + 32)
            sine, cosine = angle_rows(coarse_ref, fine_ref, block, at)
            rows = rows_of(block * (BLOCK // 32) + part, 32)
            first, second = projected_s[rows, :half], projected_s[rows, half:]
            query_out[rows, LANES : LANES + half] = ((first * sine + second * cosine) * 0.125).astype(BF16)
            query_out[rows, LANES + half :] = ((second * sine - first * cosine) * 0.125).astype(BF16)
            key_out[rows, LANES : LANES + half] = cosine.astype(BF16)
            key_out[rows, LANES + half :] = sine.astype(BF16)

    @pl.loop(0, frames // TALL)
    def _(block):
        rows = rows_of(block, TALL)
        raw_s[rows] = dot_nt(query_out[rows], key_out[...])

    key_code = item_codes(bounds_s, lax.broadcasted_iota(jnp.int32, (1, frames), 1))

    @pl.loop(0, blocks)
    def _(block):
        rows = rows_of(block, BLOCK)
        index = block * BLOCK + lax.broadcasted_iota(jnp.int32, (BLOCK, 1), 0)
        scaled = jnp.where(item_codes(bounds_s, index) == key_code, raw_s[rows], MASKED)
        weight = jnp.exp(scaled - jnp.max(scaled, axis=1, keepdims=True))
        prob_out[rows] = weight.astype(BF16)
        share = 1.0 / jnp.sum(weight, axis=1, keepdims=True)
        share_out[rows] = jnp.broadcast_to(share, (BLOCK, LANES))

    @pl.loop(0, frames // TALL)
    def _(block):
        rows = rows_of(block, TALL)
        attn_out[rows] = dot_nn(prob_out[rows], value_out[...]) * share_out[rows]


def window_place(window, frames):
    main = frames // WINDOW
    folded = window >= main
    inner = jnp.where(folded, window - main, window)
    base = inner * WINDOW + jnp.where(folded, frames + 2 * MARGIN, 0)
    start = inner * WINDOW
    return folded.astype(jnp.int32), pl.multiple_of(base, 2 * MARGIN), start, start + jnp.where(folded, frames // 2, 0)


def item_at(bounds_s, frame):
    item = jnp.int32(0)
    for other in range(1, ITEMS + 1):
        item = item + (frame >= bounds_s[other]).astype(jnp.int32)
    return item


def over_items(bounds_s, start_low, start_high, step, init):
    first_low, first_high = item_at(bounds_s, start_low), item_at(bounds_s, start_high)
    last_low = item_at(bounds_s, start_low + WINDOW - 1)
    last_high = item_at(bounds_s, start_high + WINDOW - 1)
    low = low_lanes(8)

    def one(index, carry):
        low_item, high_item = first_low + index, first_high + index
        begin = jnp.where(low, bounds_s[low_item] - start_low, bounds_s[high_item] - start_high)
        end = jnp.where(low, bounds_s[low_item + 1] - start_low, bounds_s[high_item + 1] - start_high)
        return step(begin, end, carry)

    return lax.fori_loop(0, jnp.maximum(last_low - first_low, last_high - first_high) + 1, one, init)


def inside(begin, end, base, extent):
    shape = (extent // 8, 8, LANES)
    row = base + 8 * lax.broadcasted_iota(jnp.int32, shape, 0) + lax.broadcasted_iota(jnp.int32, shape, 1)
    return ((row >= begin[None]) & (row < end[None])).reshape(extent, LANES)


def each_tap(window_ref):
    for tap in range(KERNEL):
        yield tap, window_ref[tap + 1 : tap + 1 + WINDOW].reshape(WINDOW // 8, 8, LANES)


def fill_margins(wide_s, frames):
    edge = jnp.zeros((MARGIN, LANES), F32)
    wide_s[:MARGIN] = edge
    wide_s[MARGIN + frames : 2 * MARGIN + frames] = edge
    base = frames + 3 * MARGIN
    after = base + frames // 2
    low = low_lanes(MARGIN)
    wide_s[base - MARGIN : base] = jnp.where(low, 0.0, turn(wide_s[after - MARGIN : after]))
    wide_s[after : after + MARGIN] = jnp.where(low, turn(wide_s[base : base + MARGIN]), 0.0)


def mlp_first_kernel(
    lengths_ref,
    gst_ref,
    n_ref,
    up_ref,
    table_ref,
    down_ref,
    merge_ref,
    attn_ref,
    mixed_out,
    gate_pre_out,
    gy_out,
    hat_out,
    slope_out,
    down_out,
    vectors_out,
    lines_out,
    pre_s,
    hidden_s,
    gate_slope_s,
    conv_s,
    grad_s,
    out_s,
    back_s,
    branch_s,
    gated_s,
    mix_s,
    taps_s,
    turn_s,
    tap_sum_s,
    columns_s,
    down_s,
    window_s,
    other_s,
    bounds_s,
):
    place = lax.axis_index("tm")
    frames = n_ref.shape[0]
    half = frames // 2
    blocks = frames // BLOCK
    quarters, down_rows, _ = down_out.shape
    share = down_rows // 4
    channels = quarters * share
    stride = HALF // quarters
    fill_bounds(lengths_ref, bounds_s, frames)
    for part in range(2):
        for tap in range(KERNEL):
            line = jnp.broadcast_to(table_ref[part, 8 + tap : 9 + tap], (8, LANES))
            taps_s[part, tap] = line
            turn_s[part, KERNEL - 1 - tap] = line
    tap_sum_s[...] = jnp.zeros(tap_sum_s.shape, F32)
    main, rest = table_ref[0, :8], table_ref[1, :8]

    @pl.loop(0, frames // TALL)
    def _(block):
        rows = rows_of(block, TALL)
        pre_s[rows] = dot_nn(n_ref[rows], up_ref[...])

    def stat_rows(rows):
        stats = gst_ref[rows, D:].astype(F32)
        return stats[:, 0:1] + stats[:, 1:2], stats[:, 2:3] + stats[:, 3:4]

    def conv_part(hidden, mean, rate, lines, rows, to_rows):
        hat = (hidden - mean) * rate
        hat_out[rows] = hat
        conv_s[to_rows] = (hat * lines[2:3] + lines[3:4]).astype(BF16).astype(F32)

    @pl.loop(0, frames // 64)
    def _(step):
        rows = rows_of(step, 64)
        gate, gate_slope = gelu_parts(pre_s[rows, :LANES] + main[0:1])
        hidden_s[rows] = gate
        gate_slope_s[rows] = gate_slope
        hidden, slope = gelu_parts(pre_s[rows, 2 * LANES :] + main[1:2])
        slope_out[rows] = slope
        mean, rate = stat_rows(rows)
        conv_part(hidden, mean, rate, main, rows, rows_of(step, 64, MARGIN))

    @pl.loop(0, half // 64)
    def _(step):
        low = low_lanes(64)
        mixed_bias = jnp.where(low_lanes(1), rest[0:1], rest[1:2])
        low_rows, high_rows = rows_of(step, 64), rows_of(step, 64, half)
        low_hidden, low_slope = gelu_parts(pre_s[low_rows, LANES : 2 * LANES] + mixed_bias)
        high_hidden, high_slope = gelu_parts(pre_s[high_rows, LANES : 2 * LANES] + mixed_bias)
        rows = rows_of(step, 64, frames)
        hidden_s[rows] = jnp.where(low, low_hidden, turn(high_hidden))
        gate_slope_s[rows] = jnp.where(low, low_slope, turn(high_slope))
        slope_out[rows] = jnp.where(low, turn(low_slope), high_slope)
        hidden = jnp.where(low, turn(low_hidden), high_hidden)
        low_mean, low_rate = stat_rows(low_rows)
        high_mean, high_rate = stat_rows(high_rows)
        conv_part(
            hidden,
            jnp.where(low, low_mean, high_mean),
            jnp.where(low, low_rate, high_rate),
            rest,
            rows,
            rows_of(step, 64, frames + 3 * MARGIN),
        )

    fill_margins(conv_s, frames)
    windows = (frames + half) // WINDOW
    tall = WINDOW + 2 * MARGIN

    @pl.loop(0, windows)
    def _(index):
        folded, base, start_low, start_high = window_place(index, frames)
        window = conv_s[pl.ds(base, tall)]

        def step(begin, end, total):
            window_s[...] = jnp.where(inside(begin, end, -MARGIN, tall), window, 0.0)
            part = jnp.zeros((WINDOW // 8, 8, LANES), F32)
            for tap, view in each_tap(window_s):
                part = part + view * taps_s[folded, tap][None]
            return jnp.where(inside(begin, end, 0, WINDOW), part.reshape(WINDOW, LANES), total)

        total = over_items(bounds_s, start_low, start_high, step, jnp.zeros((WINDOW, LANES), F32))
        out_s[rows_of(index, WINDOW)] = total + table_ref[folded, 4:5]

    for quarter in range(quarters):
        at = pl.ds(pl.multiple_of(quarter * stride + share * place, 16), share)
        down_s[quarter * share : (quarter + 1) * share] = down_ref[at]
    down_s[channels:] = jnp.zeros((2 * LANES - channels, D), BF16)

    @pl.loop(0, frames // TALL)
    def _(block):
        rows = rows_of(block, TALL)
        branch = dot_nt(gst_ref[rows, :D], merge_ref[D:]).astype(BF16)
        branch_s[rows] = branch
        gated_s[rows] = dot_nt(branch, down_s[...])

    def branch_part(grad_gated, rows, to_rows, sums):
        up_sum, conv_sum = sums
        gate, conv = hidden_s[rows], out_s[rows]
        gate_pre = (grad_gated * conv * gate_slope_s[rows]).astype(BF16)
        gate_pre_out[rows] = gate_pre
        grad_conv = (grad_gated * gate).astype(BF16).astype(F32)
        grad_s[to_rows] = grad_conv
        sums = (up_sum + fold_rows(gate_pre.astype(F32)), conv_sum + fold_rows(grad_conv))
        return gate * conv, sums

    zero = jnp.zeros((8, LANES), F32)

    def main_branch(step, sums):
        rows = rows_of(step, 64)
        gated, sums = branch_part(gated_s[rows, :LANES], rows, rows_of(step, 64, MARGIN), sums)
        mix_s[rows, :LANES] = gated.astype(BF16)
        return sums

    def rest_branch(step, sums):
        low = low_lanes(64)
        low_rows, high_rows = rows_of(step, 64), rows_of(step, 64, half)
        grad_gated = jnp.where(low, gated_s[low_rows, LANES:], turn(gated_s[high_rows, LANES:]))
        rows = rows_of(step, 64, frames)
        gated, sums = branch_part(grad_gated, rows, rows_of(step, 64, frames + 3 * MARGIN), sums)
        mix_s[low_rows, LANES:] = jnp.where(low, gated, turn(attn_ref[low_rows])).astype(BF16)
        mix_s[high_rows, LANES:] = jnp.where(low, turn(gated), turn(attn_ref[high_rows])).astype(BF16)
        return sums

    main_up, main_conv = lax.fori_loop(0, frames // 64, main_branch, (zero, zero))
    rest_up, rest_conv = lax.fori_loop(0, half // 64, rest_branch, (zero, zero))
    fill_margins(grad_s, frames)

    ones = jnp.ones((16, frames), BF16)
    lines_out[0:1] = dot_nn(ones, branch_s[...])[0:1]
    lines_out[1:2] = dot_nn(ones, gst_ref[:, :D])[0:1]
    lines_out[2:8] = jnp.zeros((6, D), F32)
    grad_down = dot_tn(mix_s[...], branch_s[...])
    for quarter in range(quarters):
        for tile in range(4):
            down_out[quarter, tile * share : (tile + 1) * share] = grad_down[
                quarter * share : (quarter + 1) * share, tile * LANES : (tile + 1) * LANES
            ].astype(BF16)

    @pl.loop(0, windows)
    def _(index):
        folded, base, start_low, start_high = window_place(index, frames)
        forward = conv_s[pl.ds(base, tall)]
        backward = grad_s[pl.ds(base, tall)]

        def step(begin, end, total):
            kept = inside(begin, end, -MARGIN, tall)
            own = jnp.where(kept, backward, 0.0)
            window_s[...] = own
            other_s[...] = jnp.where(kept, forward, 0.0)
            part = jnp.zeros((WINDOW // 8, 8, LANES), F32)
            for tap, view in each_tap(window_s):
                part = part + view * turn_s[folded, tap][None]
            centre = own[MARGIN : MARGIN + WINDOW].reshape(WINDOW // 8, 8, LANES)
            for tap, view in each_tap(other_s):
                tap_sum_s[folded, tap] += jnp.sum(view * centre, axis=0)
            return jnp.where(inside(begin, end, 0, WINDOW), part.reshape(WINDOW, LANES), total)

        back_s[rows_of(index, WINDOW)] = over_items(
            bounds_s, start_low, start_high, step, jnp.zeros((WINDOW, LANES), F32)
        )

    lane = lax.broadcasted_iota(jnp.int32, (64, LANES), 1)

    def norm_part(rows, lines, sums):
        gain_sum, bias_sum = sums
        back, hat = back_s[rows], hat_out[rows]
        grad = back * lines[2:3]
        gy_out[rows] = grad
        along = back * hat
        return grad, along * lines[2:3], (gain_sum + fold_rows(along), bias_sum + fold_rows(back))

    def two_columns(plain, along):
        plain = jnp.sum(plain, axis=-1, keepdims=True)
        along = jnp.sum(along, axis=-1, keepdims=True)
        return jnp.where(lane == 0, plain, jnp.where(lane == 1, along, 0.0))

    def main_norm(step, sums):
        rows = rows_of(step, 64)
        plain, along, sums = norm_part(rows, main, sums)
        columns_s[rows] = two_columns(plain, along)
        return sums

    def rest_norm(step, sums):
        low = low_lanes(64)
        plain, along, sums = norm_part(rows_of(step, 64, frames), rest, sums)
        columns_s[rows_of(step, 64)] += two_columns(jnp.where(low, plain, 0.0), jnp.where(low, along, 0.0))
        columns_s[rows_of(step, 64, half)] += two_columns(
            jnp.where(low, 0.0, plain), jnp.where(low, 0.0, along)
        )
        return sums

    main_gain, main_bias = lax.fori_loop(0, frames // 64, main_norm, (zero, zero))
    rest_gain, rest_bias = lax.fori_loop(0, half // 64, rest_norm, (zero, zero))

    totals = jnp.concatenate(
        [jnp.transpose(columns_s[block * BLOCK : (block + 1) * BLOCK])[:2] for block in range(blocks)], axis=0
    )
    high = totals.astype(BF16)
    low_part = (totals - high.astype(F32)).astype(BF16)
    for block in range(blocks):
        mixed_out[block, :BLOCK] = mix_s[block * BLOCK : (block + 1) * BLOCK]
        mixed_out[block, BLOCK:, :LANES] = high
        mixed_out[block, BLOCK:, LANES:] = low_part

    def vectors(part, lines):
        taps = jnp.sum(tap_sum_s[part], axis=1)[:KERNEL]
        stacked = jnp.concatenate([taps] + [one_row(line) for line in lines], axis=0)
        if part:
            stacked = stacked + turn(stacked)
        return jnp.transpose(
            jnp.concatenate([stacked, jnp.zeros((LANES - stacked.shape[0], LANES), F32)], axis=0)
        )

    vectors_out[:LANES] = vectors(0, (main_conv, main_gain, main_bias, main_up))
    vectors_out[LANES:] = vectors(1, (rest_conv, rest_gain, rest_bias, rest_up))[: channels - LANES]


def attend_back_kernel(
    gst_ref,
    n_ref,
    hat_ref,
    gain_ref,
    q_position_ref,
    query_ref,
    key_ref,
    value_ref,
    prob_ref,
    attn_ref,
    share_ref,
    merge_ref,
    head_ref,
    pos_ref,
    qkv_ref,
    coarse_ref,
    fine_ref,
    down_ref,
    branch_out,
    total_out,
    pack_out,
    lines_out,
    grad_s,
    score_s,
    raw_s,
    query_s,
    projected_s,
    position_s,
    parts_s,
    norm_s,
):
    place = lax.axis_index("tm")
    frames = n_ref.shape[0]
    blocks = frames // BLOCK
    half = D // 2
    head = jnp.concatenate(
        [head_ref[pl.ds(pl.multiple_of(place * HEAD, HEAD), HEAD)], jnp.zeros((LANES - HEAD, D), BF16)], axis=0
    )

    @pl.loop(0, frames // TALL)
    def _(block):
        rows = rows_of(block, TALL)
        branch = dot_nt(gst_ref[rows, :D], merge_ref[:D]).astype(BF16)
        branch_out[rows] = branch
        grad = (dot_nt(branch, head) * share_ref[rows]).astype(BF16)
        grad_s[rows] = grad
        score_s[rows] = dot_nt(grad, value_ref[...])

    @pl.loop(0, blocks)
    def _(block):
        rows = rows_of(block, BLOCK)
        delta = jnp.sum(grad_s[rows].astype(F32) * attn_ref[rows], axis=1, keepdims=True)
        raw_s[rows] = (prob_ref[rows].astype(F32) * (score_s[rows] - delta)).astype(BF16)

    @pl.loop(0, frames // TALL)
    def _(block):
        rows = rows_of(block, TALL)
        query_s[rows] = dot_nn(raw_s[rows], key_ref[...])

    @pl.loop(0, blocks)
    def _(block):
        for part in range(BLOCK // 32):
            at = slice(part * 32, part * 32 + 32)
            sine, cosine = angle_rows(coarse_ref, fine_ref, block, at)
            rows = rows_of(block * (BLOCK // 32) + part, 32)
            first = query_s[rows, LANES : LANES + half] * 0.125
            second = query_s[rows, LANES + half :] * 0.125
            projected_s[rows, :half] = (first * sine - second * cosine).astype(BF16)
            projected_s[rows, half:] = (first * cosine + second * sine).astype(BF16)

    @pl.loop(0, frames // TALL)
    def _(block):
        rows = rows_of(block, TALL)
        position_s[rows] = dot_nn(projected_s[rows], pos_ref[...])

    zero = jnp.zeros((8, LANES), F32)

    def query_step(step, sums):
        content_sum, position_sum = sums
        rows = rows_of(step, 64)
        content, position = query_s[rows, :LANES] * 0.125, position_s[rows]
        parts_s[rows, :LANES] = (content + position).astype(BF16)
        return content_sum + fold_rows(content), position_sum + fold_rows(position)

    content_sum, position_sum = lax.fori_loop(0, frames // 64, query_step, (zero, zero))
    grad_key = dot_tn(query_ref[:, :LANES], raw_s[...])
    grad_value = dot_tn(grad_s[...], prob_ref[...])
    for block in range(blocks):
        at = slice(block * BLOCK, (block + 1) * BLOCK)
        parts_s[at, LANES : 2 * LANES] = jnp.transpose(grad_key[:, at]).astype(BF16)
        parts_s[at, 2 * LANES :] = jnp.transpose(grad_value[:, at]).astype(BF16)
    grads = [
        dot_tn(parts_s[:, :LANES], n_ref[...]),
        dot_nn(grad_key.astype(BF16), n_ref[...]),
        dot_nn(grad_value.astype(BF16), n_ref[...]),
        dot_tn(q_position_ref[...], projected_s[...]),
    ]
    for quarter in range(pack_out.shape[0]):
        lanes = slice(quarter * LANES, (quarter + 1) * LANES)
        for kind in range(4):
            pack_out[quarter, kind * HEAD : (kind + 1) * HEAD] = grads[kind][:HEAD, lanes].astype(BF16)
    spare = 4 * HEAD + down_ref.shape[1]
    pack_out[:, 4 * HEAD : spare] = down_ref[...]
    pack_out[:, spare:] = jnp.zeros((pack_out.shape[0], pack_out.shape[1] - spare, LANES), BF16)

    @pl.loop(0, frames // TALL)
    def _(block):
        rows = rows_of(block, TALL)
        norm_s[rows] = dot_nt(parts_s[rows], qkv_ref[...])

    gain = line_of(gain_ref)
    wide_zero = jnp.zeros((8, D), F32)

    def norm_step(step, sums):
        gain_sum, bias_sum = sums
        rows = rows_of(step, 32)
        grad = norm_s[rows]
        total_out[rows] = (grad * gain).astype(BF16)
        return gain_sum + fold_rows(grad * hat_ref[rows].astype(F32)), bias_sum + fold_rows(grad)

    gain_sum, bias_sum = lax.fori_loop(0, frames // 32, norm_step, (wide_zero, wide_zero))
    lane = lax.broadcasted_iota(jnp.int32, (1, LANES), 1)

    def own_lanes(sums):
        line = one_row(sums)
        line = line + turn(line)
        tiles = [
            jnp.where(lax.div(tile * LANES + lane, HEAD) == place, line, 0.0) for tile in range(D // LANES)
        ]
        return jnp.concatenate(tiles, axis=1)

    lines_out[...] = jnp.concatenate(
        [
            one_row(gain_sum),
            one_row(bias_sum),
            own_lanes(content_sum),
            own_lanes(position_sum),
            jnp.zeros((4, D), F32),
        ],
        axis=0,
    )


def mlp_second_kernel(
    gst_ref,
    mixed_ref,
    n_ref,
    norm_hat_ref,
    gain_ref,
    up_ref,
    gate_pre_ref,
    gy_ref,
    hat_ref,
    slope_ref,
    vectors_ref,
    first_lines_ref,
    head_lines_ref,
    other_ref,
    same_out,
    apart_out,
    pack_0,
    pack_1,
    pack_2,
    pack_3,
    pre_s,
    columns_s,
    norm_s,
    grad_up_s,
    lines_s,
    up_columns_s,
):
    packs = (pack_0, pack_1, pack_2, pack_3)
    stream = lax.axis_index("stream")
    place = lax.axis_index("tm")
    frames = n_ref.shape[0]
    half = frames // 2
    blocks = frames // BLOCK
    quarters = len(packs)
    channels = vectors_ref.shape[0]
    share = channels // quarters
    totals = jnp.zeros((2 * blocks, LANES), F32)
    for source in range(mixed_ref.shape[0]):
        both = mixed_ref[source, BLOCK:].astype(F32)
        totals = totals + (both[:, :LANES] + both[:, LANES:])
    totals = totals * (1.0 / HALF)
    columns = jnp.transpose(jnp.concatenate([totals, jnp.zeros((LANES - 2 * blocks, LANES), F32)], axis=0))
    for block in range(blocks):
        at = slice(block * BLOCK, (block + 1) * BLOCK)
        stats = gst_ref[at, D:].astype(F32)
        rate = stats[:, 2:3] + stats[:, 3:4]
        lane = lax.broadcasted_iota(jnp.int32, (BLOCK, LANES), 1)
        kept = jnp.where(lane == 0, columns[:, 2 * block : 2 * block + 1], rate)
        columns_s[at] = jnp.where(lane == 1, columns[:, 2 * block + 1 : 2 * block + 2], kept)

    def pre_part(rows, plain, along, rate, up_sum):
        grad = rate * (gy_ref[rows] - plain - hat_ref[rows] * along)
        pre = (grad * slope_ref[rows]).astype(BF16).astype(F32)
        return pre, up_sum + fold_rows(pre)

    def main_step(step, up_sum):
        rows = rows_of(step, 64)
        table = columns_s[rows]
        pre, up_sum = pre_part(rows, table[:, 0:1], table[:, 1:2], table[:, 2:3], up_sum)
        pre_s[rows, :LANES] = gate_pre_ref[rows]
        pre_s[rows, 2 * LANES :] = pre.astype(BF16)
        return up_sum

    def rest_step(step, up_sum):
        low = low_lanes(64)
        low_rows, high_rows, rows = rows_of(step, 64), rows_of(step, 64, half), rows_of(step, 64, frames)
        low_table, high_table = columns_s[low_rows], columns_s[high_rows]
        plain, along, rate = [
            jnp.where(low, low_table[:, item : item + 1], high_table[:, item : item + 1]) for item in range(3)
        ]
        pre, up_sum = pre_part(rows, plain, along, rate, up_sum)
        gate_pre = gate_pre_ref[rows].astype(F32)
        pre_s[low_rows, LANES : 2 * LANES] = jnp.where(low, gate_pre, turn(pre)).astype(BF16)
        pre_s[high_rows, LANES : 2 * LANES] = jnp.where(low, turn(gate_pre), pre).astype(BF16)
        return up_sum

    zero = jnp.zeros((8, LANES), F32)
    main_up = lax.fori_loop(0, frames // 64, main_step, zero, unroll=4)
    rest_up = lax.fori_loop(0, half // 64, rest_step, zero, unroll=4)

    @pl.loop(0, frames // TALL)
    def _(block):
        rows = rows_of(block, TALL)
        norm_s[rows] = dot_nt(pre_s[rows], up_ref[...])

    gain = line_of(gain_ref)
    wide_zero = jnp.zeros((8, D), F32)

    def norm_step(block, sums):
        gain_sum, bias_sum = sums
        rows = rows_of(block, BLOCK)
        grad = norm_s[rows]
        total = (grad * gain + other_ref[rows].astype(F32)).astype(BF16)
        apart = lax.bitwise_xor(block, place)
        slot = lax.div(apart, 2)

        @pl.when(lax.rem(apart, 2) == 0)
        def _():
            same_out[slot] = total

        @pl.when(lax.rem(apart, 2) == 1)
        def _():
            apart_out[slot] = total

        return gain_sum + fold_rows(grad * norm_hat_ref[rows].astype(F32)), bias_sum + fold_rows(grad)

    gain_sum, bias_sum = lax.fori_loop(0, blocks, norm_step, (wide_zero, wide_zero))
    grad_up_s[...] = dot_tn(pre_s[...], n_ref[...])
    rest_line = one_row(rest_up)
    up_columns_s[:LANES] = jnp.transpose(jnp.broadcast_to(one_row(main_up), (LANES, LANES)))
    up_columns_s[LANES:] = jnp.transpose(jnp.broadcast_to(rest_line + turn(rest_line), (LANES, LANES)))[:LOW]
    first_device = (place == 0).astype(F32)
    lines_s[...] = jnp.concatenate(
        [
            head_lines_ref[0:2],
            one_row(gain_sum),
            one_row(bias_sum),
            head_lines_ref[2:4],
            first_lines_ref[0:2] * first_device,
            jnp.zeros((8, D), F32),
        ],
        axis=0,
    )
    gate_at = KERNEL + 3
    lane = lax.broadcasted_iota(jnp.int32, (share, LANES), 1)
    for apart, pack_out in enumerate(packs):
        quarter = lax.bitwise_xor(stream, jnp.int32(apart))
        lanes = pl.ds(pl.multiple_of(quarter * LANES, LANES), LANES)
        pack_out[:channels] = grad_up_s[:channels, lanes].astype(BF16)
        pack_out[channels : channels + LANES] = grad_up_s[2 * LANES :, lanes].astype(BF16)
        pack_out[channels + LANES : 2 * channels] = grad_up_s[channels : 2 * LANES, lanes].astype(BF16)
        table = vectors_ref[pl.ds(pl.multiple_of(quarter * share, 8), share)]
        for other in range(2):
            at = pl.ds(pl.multiple_of((2 * lax.rem(quarter, 2) + other) * share, 8), share)
            column = jnp.where(
                quarter < quarters // 2, vectors_ref[at][:, gate_at : gate_at + 1], up_columns_s[at][:, 0:1]
            )
            table = jnp.where(lane == gate_at + other, column, table)
        pack_out[2 * channels : 2 * channels + share] = table.astype(BF16)
        pack_out[2 * channels + share :] = lines_s[:, lanes].astype(BF16)


def output_kernel(
    x_ref, mixed_ref, head_ref, down_ref, down_bias_ref, merge_ref, merge_bias_ref, out_ref, joined_out
):
    sources = mixed_ref.shape[0]
    rows = x_ref.shape[0]
    channels = HALF // sources
    share = channels // 4
    attn_parts = []
    branch_attn = jnp.zeros((rows, D), F32)
    branch_mlp = jnp.zeros((rows, D), F32)
    for source in range(sources):
        attn = turn(mixed_ref[source, :rows, LANES:].astype(F32))[:, :HEAD].astype(BF16)
        attn_parts.append(attn)
        branch_attn = branch_attn + dot_nn(attn, head_ref[source * HEAD : (source + 1) * HEAD])
        down = jnp.concatenate(
            [down_ref[(part * sources + source) * share : (part * sources + source + 1) * share] for part in range(4)],
            axis=0,
        )
        branch_mlp = branch_mlp + dot_nn(mixed_ref[source, :rows, :channels], down)
    joined = jnp.concatenate(
        [branch_attn.astype(BF16), (branch_mlp + line_of(down_bias_ref)).astype(BF16)], axis=1
    )
    result = x_ref[...].astype(F32) + dot_nn(joined, merge_ref[...]) + line_of(merge_bias_ref)
    out_ref[...] = result.astype(BF16)
    turned = jnp.transpose(joined.astype(F32))
    heads = jnp.transpose(jnp.concatenate(attn_parts, axis=1).astype(F32))
    merge_share = turned.shape[0] // (4 * sources)
    head_share = heads.shape[0] // (4 * sources)
    used = 4 * (merge_share + head_share)
    for target in range(sources):
        for part in range(4):
            at = (part * sources + target) * merge_share
            joined_out[target, part * merge_share : (part + 1) * merge_share] = turned[
                at : at + merge_share
            ].astype(BF16)
            at = (part * sources + target) * head_share
            to = 4 * merge_share + part * head_share
            joined_out[target, to : to + head_share] = heads[at : at + head_share].astype(BF16)
        joined_out[target, used:] = jnp.zeros((joined_out.shape[1] - used, rows), BF16)


def merge_kernel(joined_ref, gst_ref, branch_ref, pack_0, pack_1, pack_2, pack_3, merge_s, head_s):
    stream = lax.axis_index("stream")
    sources, _, rows = joined_ref.shape
    merge_rows = 2 * D // sources
    head_rows = D // sources
    grad_merge = jnp.zeros((merge_rows, D), F32)
    grad_head = jnp.zeros((head_rows, D), F32)
    for source in range(sources):
        at = slice(source * rows, (source + 1) * rows)
        grad_merge = grad_merge + dot_nn(joined_ref[source, :merge_rows], gst_ref[at, :D])
        grad_head = grad_head + dot_nn(joined_ref[source, merge_rows : merge_rows + head_rows], branch_ref[at])
    merge_s[...] = grad_merge
    head_s[...] = grad_head
    for apart, pack_out in enumerate((pack_0, pack_1, pack_2, pack_3)):
        quarter = lax.bitwise_xor(stream, jnp.int32(apart))
        for grad_s, base in ((merge_s, 0), (head_s, merge_rows)):
            share = grad_s.shape[0] // 4
            at = pl.ds(pl.multiple_of(quarter * share, share), share)
            for tile in range(4):
                to = base + tile * share
                pack_out[to : to + share] = grad_s[at, tile * LANES : (tile + 1) * LANES].astype(BF16)


def pair_kernel(same_ref, other_ref, *out_refs):
    for slot, out_ref in enumerate(out_refs):
        out_ref[...] = (same_ref[slot].astype(F32) + other_ref[slot].astype(F32)).astype(BF16)


def frames_kernel(x_ref, cot_ref, *refs):
    total_refs, out_ref = refs[:-1], refs[-1]
    for part in range(x_ref.shape[0] // 32):
        rows = slice(part * 32, part * 32 + 32)
        inputs = x_ref[rows].astype(F32)
        mean = jnp.mean(inputs, axis=-1, keepdims=True)
        centred = inputs - mean
        rate = lax.rsqrt(jnp.mean(centred * centred, axis=-1, keepdims=True) + EPS)
        hat = centred * rate
        grad = total_refs[0][rows].astype(F32)
        for total_ref in total_refs[1:]:
            grad = grad + total_ref[rows].astype(F32)
        plain = jnp.mean(grad, axis=-1, keepdims=True)
        along = jnp.mean(grad * hat, axis=-1, keepdims=True)
        out_ref[rows] = cot_ref[rows].astype(F32) + rate * (grad - plain - hat * along)


def add_kernel(*refs):
    out_ref = refs[-1]
    count = (len(refs) - 1) // 2
    split = refs[0].shape[0]
    for part, rows in ((refs[:count], slice(0, split)), (refs[count:-1], slice(split, out_ref.shape[0]))):
        total = part[0][...].astype(F32)
        for ref in part[1:]:
            total = total + ref[...].astype(F32)
        out_ref[rows] = total.astype(BF16)


def early_kernel(all_ref, qkv_out, pos_out, down_out):
    sources = all_ref.shape[0]
    share = HALF // (4 * sources)
    for kind in range(4):
        lines = jnp.transpose(
            jnp.concatenate(
                [all_ref[source, kind * HEAD : (kind + 1) * HEAD] for source in range(sources)], axis=0
            ).astype(F32)
        )
        if kind < 3:
            qkv_out[:, kind * D : (kind + 1) * D] = lines
        else:
            pos_out[...] = lines
    for source in range(sources):
        for tile in range(4):
            at = 4 * HEAD + tile * share
            down_out[source * share : (source + 1) * share, tile * LANES : (tile + 1) * LANES] = all_ref[
                source, at : at + share
            ].astype(F32)


def late_kernel(*refs):
    part_refs = refs[:HEADS]
    (
        attn_gain_out,
        attn_bias_out,
        mlp_gain_out,
        mlp_bias_out,
        content_out,
        position_out,
        outw_out,
        up_out,
        up_bias_out,
        gain_out,
        bias_out,
        taps_out,
        conv_bias_out,
        down_bias_out,
        merge_out,
        merge_bias_out,
        all_s,
    ) = refs[HEADS:]
    place = lax.axis_index("tm")
    sources = all_s.shape[0]
    for apart, part_ref in enumerate(part_refs):
        all_s[lax.bitwise_xor(jnp.int32(apart), place)] = part_ref[...]
    channels = HALF // sources
    share = channels // 4

    def lines_at(base, size):
        return jnp.concatenate([all_s[source, base : base + size] for source in range(sources)], axis=0).astype(F32)

    for half in range(2):
        for group in range(4):
            at = half * HALF + group * sources * share
            up_out[:, at : at + sources * share] = jnp.transpose(
                lines_at(half * channels + group * share, share)
            )
    table = jnp.transpose(lines_at(2 * channels, share))
    taps_out[...] = table[:KERNEL]
    conv_bias_out[...] = table[KERNEL]
    gain_out[...] = table[KERNEL + 1]
    bias_out[...] = table[KERNEL + 2]
    wide = sources * share
    up_bias_out[:wide] = table[KERNEL + 3]
    up_bias_out[wide:] = table[KERNEL + 4]
    base = 2 * channels + share
    lines = all_s[0, base : base + 16].astype(F32)
    for source in range(1, sources):
        lines = lines + all_s[source, base : base + 16].astype(F32)
    outs = (attn_gain_out, attn_bias_out, mlp_gain_out, mlp_bias_out, content_out, position_out, down_bias_out, merge_bias_out)
    for line, out in enumerate(outs):
        out[...] = lines[line]
    base = base + 16
    merge_share = 2 * D // (4 * sources)
    head_share = D // (4 * sources)
    for source in range(sources):
        for tile in range(4):
            lanes = slice(tile * LANES, (tile + 1) * LANES)
            at = base + tile * merge_share
            merge_out[source * merge_share : (source + 1) * merge_share, lanes] = all_s[
                source, at : at + merge_share
            ].astype(F32)
            at = base + 4 * merge_share + tile * head_share
            outw_out[source * head_share : (source + 1) * head_share, lanes] = all_s[
                source, at : at + head_share
            ].astype(F32)


def moved(block, axis, bits):
    count = lax.axis_size(axis)
    return lax.ppermute(block, axis, [(index, index ^ bits) for index in range(count)])


def spread(block):
    near = [block] + [moved(block, "tm", bits) for bits in range(2, lax.axis_size("tm"), 2)]
    far = [moved(part, "tm", 1) for part in near]
    return [part for pair in zip(near, far) for part in pair]


def head_device(
    frames,
    lengths,
    cotangent,
    ln_attn_gain,
    ln_attn_bias,
    ln_mlp_gain,
    ln_mlp_bias,
    qkv_weight,
    content_bias,
    position_bias,
    pos_weight,
    out_weight,
    up_weight,
    up_bias,
    gate_norm_gain,
    gate_norm_bias,
    conv_kernel,
    conv_bias,
    down_weight,
    down_bias,
    merge_weight,
    merge_bias,
):
    count = lax.axis_size("tm")
    quarters = lax.axis_size("stream")
    own = frames.shape[1]
    total = own * count
    folded = total + total // 2
    padded = folded + 4 * MARGIN
    share = HALF // (quarters * count)
    channels = HALF // count
    quarter = D // quarters
    own_frames = frames[0]
    own_cotangent = cotangent[0]

    blocks = spread(own_frames)
    (gst_own,) = kernel_call(stats_kernel, [((own, D + LANES), BF16)], "vvvvhv", [((own, HALF), F32)], micros=4)(
        own_frames, own_cotangent, ln_mlp_gain, ln_mlp_bias, up_weight, up_bias
    )
    gst = lax.all_gather(gst_own, "tm", axis=0, tiled=True)
    up_own, table, qkv_own, pos_own, bias_own = kernel_call(
        select_kernel,
        [
            ((D, 3 * LANES), BF16),
            ((2, 8 + KERNEL + 1, LANES), F32),
            ((D, 3 * LANES), BF16),
            ((D, LANES), BF16),
            ((8, LANES), F32),
        ],
        10 * "v",
    )(
        up_weight,
        up_bias,
        gate_norm_gain,
        gate_norm_bias,
        conv_bias,
        conv_kernel,
        qkv_weight,
        pos_weight,
        content_bias,
        position_bias,
    )
    frequency = jnp.exp(jnp.arange(D // 2, dtype=F32) * (-2.0 * math.log(10000.0) / D))
    coarse = jnp.arange(0, total, BLOCK, dtype=F32)[:, None] * frequency[None]
    fine = jnp.arange(BLOCK, dtype=F32)[:, None] * frequency[None]
    coarse_table = jnp.concatenate([jnp.sin(coarse), jnp.cos(coarse)], axis=1)
    fine_table = jnp.concatenate([jnp.sin(fine), jnp.cos(fine)], axis=1)

    n_attn, n_mlp, hat, q_position, query, key, value, prob, attn, row_share = kernel_call(
        attend_kernel,
        [
            ((total, D), BF16),
            ((total, D), BF16),
            ((total, D), BF16),
            ((total, LANES), BF16),
            ((total, LANES + D), BF16),
            ((total, LANES + D), BF16),
            ((total, LANES), BF16),
            ((total, total), BF16),
            ((total, LANES), F32),
            ((total, LANES), F32),
        ],
        "s" + 17 * "v",
        [((total, 3 * LANES), F32), ((total, D), F32), ((total, total), F32)],
        bounds=True,
        micros=16,
    )(
        lengths,
        *blocks,
        ln_attn_gain,
        ln_attn_bias,
        ln_mlp_gain,
        ln_mlp_bias,
        qkv_own,
        pos_own,
        bias_own,
        coarse_table,
        fine_table,
    )

    mixed, gate_pre, grad_y, gate_hat, slope, down_pack, vectors, first_lines = kernel_call(
        mlp_first_kernel,
        [
            ((count, own + 16, 2 * LANES), BF16),
            ((folded, LANES), BF16),
            ((folded, LANES), F32),
            ((folded, LANES), F32),
            ((folded, LANES), F32),
            ((quarters, 4 * share, LANES), BF16),
            ((channels, LANES), F32),
            ((8, D), F32),
        ],
        "s" + 7 * "v",
        [
            ((total, 3 * LANES), F32),
            ((folded, LANES), F32),
            ((folded, LANES), F32),
            ((padded, LANES), F32),
            ((padded, LANES), F32),
            ((folded, LANES), F32),
            ((folded, LANES), F32),
            ((total, D), BF16),
            ((total, 2 * LANES), F32),
            ((total, 2 * LANES), BF16),
            ((2, 32, 8, LANES), F32),
            ((2, 32, 8, LANES), F32),
            ((2, 32, 8, LANES), F32),
            ((total, LANES), F32),
            ((2 * LANES, D), BF16),
            ((WINDOW + 2 * MARGIN, LANES), F32),
            ((WINDOW + 2 * MARGIN, LANES), F32),
        ],
        bounds=True,
        micros=28,
    )(lengths, gst, n_mlp, up_own, table, down_weight, merge_weight, attn)
    mixed_own = lax.all_to_all(mixed, "tm", 0, 0, tiled=True)

    branch, from_attn, head_pack, head_lines = kernel_call(
        attend_back_kernel,
        [
            ((total, D), BF16),
            ((total, D), BF16),
            ((quarters, 512, LANES), BF16),
            ((8, D), F32),
        ],
        18 * "v",
        [
            ((total, LANES), BF16),
            ((total, total), F32),
            ((total, total), BF16),
            ((total, LANES + D), F32),
            ((total, D), BF16),
            ((total, LANES), F32),
            ((total, 3 * LANES), BF16),
            ((total, D), F32),
        ],
        micros=17,
        megas=40,
    )(
        gst,
        n_attn,
        hat,
        ln_attn_gain,
        q_position,
        query,
        key,
        value,
        prob,
        attn,
        row_share,
        merge_weight,
        out_weight,
        pos_own,
        qkv_own,
        coarse_table,
        fine_table,
        down_pack,
    )
    head_part = lax.psum_scatter(head_pack, "stream", scatter_dimension=0)
    head_all = lax.all_gather(head_part, "tm", axis=0)

    out_rows, joined = kernel_call(
        output_kernel,
        [((own, D), BF16), ((count, 256, own), BF16)],
        "vvvvvvv",
    )(own_frames, mixed_own, out_weight, down_weight, down_bias, merge_weight, merge_bias)
    joined_all = lax.all_to_all(joined, "tm", 0, 0, tiled=True)

    pack_rows = 9 * share + 16
    same, apart, *up_packs = kernel_call(
        mlp_second_kernel,
        [((count // 2, own, D), BF16)] * 2 + [((pack_rows, LANES), BF16)] * quarters,
        14 * "v",
        [
            ((total, 3 * LANES), BF16),
            ((total, LANES), F32),
            ((total, D), F32),
            ((3 * LANES, D), F32),
            ((16, D), F32),
            ((channels, LANES), F32),
        ],
        micros=10,
    )(
        gst,
        mixed_own,
        n_mlp,
        hat,
        ln_mlp_gain,
        up_own,
        gate_pre,
        grad_y,
        gate_hat,
        slope,
        vectors,
        first_lines,
        head_lines,
        from_attn,
    )
    sibling = moved(apart, "tm", 1)
    up_parts = [up_packs[0]] + [moved(up_packs[bits], "stream", bits) for bits in range(1, quarters)]
    merge_rows = 3 * D // count
    merge_packs = kernel_call(
        merge_kernel,
        [((merge_rows, LANES), BF16)] * quarters,
        "vvv",
        [((2 * D // count, D), F32), ((D // count, D), F32)],
        micros=3,
    )(joined_all, gst, branch)
    merge_parts = [merge_packs[0]] + [moved(merge_packs[bits], "stream", bits) for bits in range(1, quarters)]
    pairs = kernel_call(pair_kernel, [((own, D), BF16)] * (count // 2), "vv", micros=1)(same, sibling)
    sums = [pairs[0]] + [moved(pairs[slot], "tm", 2 * slot) for slot in range(1, count // 2)]
    (late_part,) = kernel_call(
        add_kernel, [((pack_rows + merge_rows, LANES), BF16)], 2 * quarters * "v", micros=1
    )(*up_parts, *merge_parts)
    late_parts = spread(late_part)
    (grad_frames,) = kernel_call(frames_kernel, [((own, D), F32)], (2 + count // 2) * "v")(
        own_frames, own_cotangent, *sums
    )
    grad_qkv, grad_pos, grad_down = kernel_call(
        early_kernel,
        [((quarter, 3 * D), F32), ((quarter, D), F32), ((HALF // quarters, D), F32)],
        "v",
    )(head_all)
    late = kernel_call(
        late_kernel,
        [((quarter,), F32)] * 6
        + [
            ((quarter, D), F32),
            ((quarter, 2 * HALF), F32),
            ((2 * HALF // quarters,), F32),
            ((HALF // quarters,), F32),
            ((HALF // quarters,), F32),
            ((KERNEL, HALF // quarters), F32),
            ((HALF // quarters,), F32),
            ((quarter,), F32),
            ((2 * D // quarters, D), F32),
            ((quarter,), F32),
        ],
        count * "v",
        [((count,) + late_part.shape, BF16)],
        micros=3,
    )(*late_parts)
    return (
        (out_rows[None], grad_frames[None])
        + tuple(late[:4])
        + (grad_qkv,)
        + tuple(late[4:6])
        + (grad_pos,)
        + tuple(late[6:13])
        + (grad_down,)
        + tuple(late[13:])
    )


def per_device(*operands):
    fits = (
        lax.axis_size("tm") == HEADS
        and lax.axis_size("stream") * LANES == D
        and operands[0].shape[1] == BLOCK
    )
    return head_device(*operands) if fits else frame_device(*operands)


def solution(mesh):
    return jax.shard_map(
        per_device,
        mesh=mesh,
        in_specs=(
            P("stream", "tm", None),
            P("stream", None),
            P("stream", "tm", None),
            P(),
            P(),
            P(),
            P(),
            P(),
            P(),
            P(),
            P(),
            P(),
            P(),
            P(),
            P(),
            P(),
            P(),
            P(),
            P(),
            P(),
            P(),
            P(),
        ),
        out_specs=(
            P("stream", "tm", None),
            P("stream", "tm", None),
            P("stream"),
            P("stream"),
            P("stream"),
            P("stream"),
            P("stream", None),
            P("stream"),
            P("stream"),
            P("stream", None),
            P("stream", None),
            P("stream", None),
            P("stream"),
            P("stream"),
            P("stream"),
            P(None, "stream"),
            P("stream"),
            P("stream", None),
            P("stream"),
            P("stream", None),
            P("stream"),
        ),
        check_vma=False,
    )
```

```python
import math

import jax
import jax.numpy as jnp
from jax import lax
from jax.experimental import pallas as pl
from jax.experimental.pallas import tpu as pltpu
from jax.sharding import PartitionSpec as P

D = 512
HEADS = 8
HEAD = 64
KERNEL = 31
ITEMS = 5
HALF = 1536


EPS = 1e-05
MASKED = -1e30


def extended(block, sides, width):
    for axis, dim in sides:
        count = lax.axis_size(axis)
        forward = [(i, i + 1) for i in range(count - 1)]
        backward = [(target, source) for source, target in forward]
        low = lax.ppermute(
            lax.slice_in_dim(block, block.shape[dim] - width, None, axis=dim), axis, forward
        )
        high = lax.ppermute(lax.slice_in_dim(block, 0, width, axis=dim), axis, backward)
        block = jnp.concatenate([low, block, high], axis=dim)
    return block


def norm_rows(inputs, scale_row, shift_row):
    row_mean = jnp.mean(inputs, axis=-1, keepdims=True)
    centred = inputs - row_mean
    spread = jnp.mean(centred * centred, axis=-1, keepdims=True)
    return centred * lax.rsqrt(spread + EPS) * scale_row + shift_row


def gelu_exact(inputs):
    return jax.nn.gelu(inputs, approximate=False)


def frame_info(lengths, offset, extent):
    item_ends = jnp.cumsum(lengths)
    first_table = jnp.concatenate([item_ends - lengths, item_ends[-1:]])
    frame_index = offset + jnp.arange(extent, dtype=jnp.int32)
    item_of = jnp.sum((frame_index[:, None] >= item_ends[None, :]).astype(jnp.int32), axis=1)
    labels = jnp.arange(ITEMS + 1, dtype=jnp.int32)
    first_frame = jnp.sum(
        jnp.where(item_of[:, None] == labels[None, :], first_table[None, :], 0), axis=1
    )
    return (frame_index, item_of, frame_index - first_frame)


def angles(place_in):
    frequency = jnp.exp(jnp.arange(D // 2, dtype=jnp.float32) * (-2.0 * math.log(10000.0) / D))
    phase_angle = place_in.astype(jnp.float32)[:, None] * frequency[None, :]
    return (jnp.sin(phase_angle), jnp.cos(phase_angle))


def rel_query(projected, sine_rows, cosine_rows):
    half_size = projected.shape[-1] // 2
    first_half = projected[..., :half_size]
    second_half = projected[..., half_size:]
    sine_wide = sine_rows[:, None, :]
    cosine_wide = cosine_rows[:, None, :]
    return jnp.concatenate(
        [
            first_half * sine_wide + second_half * cosine_wide,
            second_half * sine_wide - first_half * cosine_wide,
        ],
        axis=-1,
    )


def step_size(extent):
    return math.gcd(extent, 512)


def score_block(q_content, q_rel, query_item, query_frame, key_block, key_start, lengths):
    extent = key_block.shape[0]
    key_frame, key_item, key_place = frame_info(lengths, key_start, extent)
    sine_rows, cosine_rows = angles(key_place)
    k_rel = jnp.concatenate([cosine_rows, sine_rows], axis=1).astype(jnp.bfloat16)
    raw_scores = jnp.einsum(
        "qhe,khe->hqk",
        q_content,
        key_block.reshape(extent, HEADS, HEAD),
        preferred_element_type=jnp.float32,
    )
    raw_scores = raw_scores + jnp.einsum(
        "qhc,kc->hqk", q_rel, k_rel, preferred_element_type=jnp.float32
    )
    allowed = (query_item[:, None] == key_item[None, :]) & (
        (query_item[:, None] < ITEMS) | (query_frame[:, None] == key_frame[None, :])
    )
    return (raw_scores, allowed, k_rel)


def block_grads(
    q_content,
    q_rel,
    query_item,
    query_frame,
    grad_out,
    log_total,
    delta_rows,
    key_block,
    value_block,
    key_start,
    lengths,
):
    extent = key_block.shape[0]
    raw_scores, allowed, k_rel = score_block(
        q_content, q_rel, query_item, query_frame, key_block, key_start, lengths
    )
    prob_rows = jnp.where(allowed[None], jnp.exp(raw_scores * 0.125 - log_total[:, :, None]), 0.0)
    grad_prob = jnp.einsum(
        "qhe,khe->hqk",
        grad_out,
        value_block.reshape(extent, HEADS, HEAD),
        preferred_element_type=jnp.float32,
    )
    grad_raw = (prob_rows * (grad_prob - delta_rows[:, :, None]) * 0.125).astype(jnp.bfloat16)
    return (prob_rows.astype(jnp.bfloat16), grad_raw, k_rel)


def frame_device(
    frames,
    lengths,
    cotangent,
    ln_attn_gain,
    ln_attn_bias,
    ln_mlp_gain,
    ln_mlp_bias,
    qkv_weight,
    content_bias,
    position_bias,
    pos_weight,
    out_weight,
    up_weight,
    up_bias,
    gate_norm_gain,
    gate_norm_bias,
    conv_kernel,
    conv_bias,
    down_weight,
    down_bias,
    merge_weight,
    merge_bias,
):
    row_count = frames.shape[1]
    cycle_size = lax.axis_size("tm")
    offset = lax.axis_index("tm") * row_count
    stream_lengths = lengths[0]
    inputs = frames[0].astype(jnp.float32)
    frame_index, item_of, place_in = frame_info(stream_lengths, offset, row_count)
    sine_rows, cosine_rows = angles(place_in)
    attn_norm, attn_pull = jax.vjp(
        norm_rows, inputs, ln_attn_gain.astype(jnp.float32), ln_attn_bias.astype(jnp.float32)
    )
    mlp_norm, mlp_pull = jax.vjp(
        norm_rows, inputs, ln_mlp_gain.astype(jnp.float32), ln_mlp_bias.astype(jnp.float32)
    )
    attn_norm_low = attn_norm.astype(jnp.bfloat16)
    mlp_norm_low = mlp_norm.astype(jnp.bfloat16)
    qkv_rows = jnp.dot(attn_norm_low, qkv_weight, preferred_element_type=jnp.float32)
    query_rows = qkv_rows[:, :D]
    key_rows = qkv_rows[:, D : 2 * D].astype(jnp.bfloat16)
    value_rows = qkv_rows[:, 2 * D :].astype(jnp.bfloat16)
    q_content = (query_rows + content_bias.astype(jnp.float32)).astype(jnp.bfloat16)
    q_position = (query_rows + position_bias.astype(jnp.float32)).astype(jnp.bfloat16)
    content_heads = q_content.reshape(row_count, HEADS, HEAD)
    position_heads = q_position.reshape(row_count, HEADS, HEAD)
    pos_heads = pos_weight.reshape(D, HEADS, HEAD)
    projected = jnp.einsum(
        "the,che->thc", position_heads, pos_heads, preferred_element_type=jnp.float32
    )
    q_rel = rel_query(projected, sine_rows, cosine_rows).astype(jnp.bfloat16)
    start_state = (
        jnp.full((HEADS, row_count), MASKED, jnp.float32),
        jnp.zeros((HEADS, row_count), jnp.float32),
        jnp.zeros((HEADS, row_count, HEAD), jnp.float32),
    )
    fold_state = start_state
    key_piece = lax.all_gather(key_rows, "tm", axis=0, tiled=True)
    value_piece = lax.all_gather(value_rows, "tm", axis=0, tiled=True)
    extent = key_piece.shape[0]
    step_rows = step_size(extent)

    def forward_one_step(inner_state, step_index):
        row_top, row_total, row_acc = inner_state
        key_block = lax.dynamic_slice_in_dim(key_piece, step_index * step_rows, step_rows, 0)
        value_block = lax.dynamic_slice_in_dim(value_piece, step_index * step_rows, step_rows, 0)
        raw_scores, allowed, k_rel = score_block(
            content_heads,
            q_rel,
            item_of,
            frame_index,
            key_block,
            step_index * step_rows,
            stream_lengths,
        )
        scaled = jnp.where(allowed[None], raw_scores * 0.125, MASKED)
        new_top = jnp.maximum(row_top, jnp.max(scaled, axis=2))
        weight = jnp.where(allowed[None], jnp.exp(scaled - new_top[:, :, None]), 0.0)
        factor = jnp.exp(row_top - new_top)
        row_total = row_total * factor + jnp.sum(weight, axis=2)
        row_acc = row_acc * factor[:, :, None] + jnp.einsum(
            "hqk,khe->hqe",
            weight.astype(jnp.bfloat16),
            value_block.reshape(step_rows, HEADS, HEAD),
            preferred_element_type=jnp.float32,
        )
        return ((new_top, row_total, row_acc), None)

    fold_state, unused = lax.scan(
        forward_one_step, fold_state, jnp.arange(extent // step_rows, dtype=jnp.int32)
    )
    row_top, row_total, row_acc = fold_state
    attn_heads = row_acc / row_total[:, :, None]
    log_total = row_top + jnp.log(row_total)
    attn_low = jnp.transpose(attn_heads, (1, 0, 2)).reshape(row_count, D).astype(jnp.bfloat16)
    branch_attn = jnp.dot(attn_low, out_weight, preferred_element_type=jnp.float32).astype(
        jnp.bfloat16
    )
    hidden_pre = jnp.dot(
        mlp_norm_low, up_weight, preferred_element_type=jnp.float32
    ) + up_bias.astype(jnp.float32)
    hidden, gelu_pull = jax.vjp(gelu_exact, hidden_pre)
    gate_half = hidden[:, :HALF]
    conv_norm, conv_pull = jax.vjp(
        norm_rows,
        hidden[:, HALF:],
        gate_norm_gain.astype(jnp.float32),
        gate_norm_bias.astype(jnp.float32),
    )
    conv_in = conv_norm.astype(jnp.bfloat16)
    half_width = KERNEL // 2
    conv_wide = extended(conv_in, (("tm", 0),), half_width)
    wide_frame, wide_item, wide_place = frame_info(
        stream_lengths, offset - half_width, row_count + 2 * half_width
    )
    kernel_rows = conv_kernel.astype(jnp.float32)
    conv_out = conv_bias.astype(jnp.float32) + jnp.zeros_like(gate_half)
    for tap_index in range(KERNEL):
        same_item = (wide_item[tap_index : tap_index + row_count] == item_of)[:, None]
        conv_out = (
            conv_out
            + jnp.where(
                same_item, conv_wide[tap_index : tap_index + row_count].astype(jnp.float32), 0.0
            )
            * kernel_rows[tap_index]
        )
    gated_low = (gate_half * conv_out).astype(jnp.bfloat16)
    branch_mlp = (
        jnp.dot(gated_low, down_weight, preferred_element_type=jnp.float32)
        + down_bias.astype(jnp.float32)
    ).astype(jnp.bfloat16)
    joined = jnp.concatenate([branch_attn, branch_mlp], axis=1)
    result = (
        inputs
        + jnp.dot(joined, merge_weight, preferred_element_type=jnp.float32)
        + merge_bias.astype(jnp.float32)
    )
    out_rows = result.astype(jnp.bfloat16)[None]
    grad_low = cotangent[0]
    grad_rows = grad_low.astype(jnp.float32)
    grad_merge_bias = jnp.sum(grad_rows, axis=0)
    grad_merge_weight = jnp.einsum(
        "tc,td->cd", joined, grad_low, preferred_element_type=jnp.float32
    )
    grad_joined = jnp.einsum(
        "td,cd->tc", grad_low, merge_weight, preferred_element_type=jnp.float32
    )
    grad_attn_branch = grad_joined[:, :D].astype(jnp.bfloat16)
    grad_mlp_branch = grad_joined[:, D:].astype(jnp.bfloat16)
    grad_down_weight = jnp.einsum(
        "tc,td->cd", gated_low, grad_mlp_branch, preferred_element_type=jnp.float32
    )
    grad_down_bias = jnp.sum(grad_mlp_branch.astype(jnp.float32), axis=0)
    grad_gated = jnp.einsum(
        "td,cd->tc", grad_mlp_branch, down_weight, preferred_element_type=jnp.float32
    )
    grad_gate_half = grad_gated * conv_out
    grad_conv_out = (grad_gated * gate_half).astype(jnp.bfloat16)
    grad_conv_rows = grad_conv_out.astype(jnp.float32)
    grad_conv_bias = jnp.sum(grad_conv_rows, axis=0)
    grad_wide = extended(grad_conv_out, (("tm", 0),), half_width)
    kernel_list = []
    grad_conv_in = jnp.zeros_like(grad_conv_rows)
    for tap_index in range(KERNEL):
        same_item = (wide_item[tap_index : tap_index + row_count] == item_of)[:, None]
        kernel_list.append(
            jnp.sum(
                jnp.where(
                    same_item, conv_wide[tap_index : tap_index + row_count].astype(jnp.float32), 0.0
                )
                * grad_conv_rows,
                axis=0,
            )
        )
        back_start = 2 * half_width - tap_index
        back_item = (wide_item[back_start : back_start + row_count] == item_of)[:, None]
        grad_conv_in = (
            grad_conv_in
            + jnp.where(
                back_item, grad_wide[back_start : back_start + row_count].astype(jnp.float32), 0.0
            )
            * kernel_rows[tap_index]
        )
    grad_conv_kernel = jnp.stack(kernel_list)
    grad_second, grad_gate_norm_gain, grad_gate_norm_bias = conv_pull(grad_conv_in)
    (grad_pre_rows,) = gelu_pull(jnp.concatenate([grad_gate_half, grad_second], axis=1))
    grad_pre = grad_pre_rows.astype(jnp.bfloat16)
    grad_up_bias = jnp.sum(grad_pre.astype(jnp.float32), axis=0)
    grad_up_weight = jnp.einsum(
        "tc,tf->cf", mlp_norm_low, grad_pre, preferred_element_type=jnp.float32
    )
    grad_mlp_norm = jnp.einsum("tf,cf->tc", grad_pre, up_weight, preferred_element_type=jnp.float32)
    grad_out_weight = jnp.einsum(
        "tc,td->cd", attn_low, grad_attn_branch, preferred_element_type=jnp.float32
    )
    grad_attn_low = jnp.einsum(
        "td,cd->tc", grad_attn_branch, out_weight, preferred_element_type=jnp.float32
    ).astype(jnp.bfloat16)
    grad_out_heads = grad_attn_low.reshape(row_count, HEADS, HEAD)
    delta_rows = jnp.sum(
        jnp.transpose(grad_out_heads.astype(jnp.float32), (1, 0, 2)) * attn_heads, axis=2
    )
    total_frames = row_count * cycle_size
    back_start_state = (
        jnp.zeros((row_count, HEADS, HEAD), jnp.float32),
        jnp.zeros((row_count, HEADS, D), jnp.float32),
        jnp.zeros((total_frames, D), jnp.float32),
        jnp.zeros((total_frames, D), jnp.float32),
    )
    back_key_piece = lax.all_gather(key_rows, "tm", axis=0, tiled=True)
    back_value_piece = lax.all_gather(value_rows, "tm", axis=0, tiled=True)
    extent = back_key_piece.shape[0]
    back_step_rows = step_size(extent)

    def back_one_step(inner_state, step_index):
        grad_content, grad_rel = inner_state
        key_block = lax.dynamic_slice_in_dim(
            back_key_piece, step_index * back_step_rows, back_step_rows, 0
        )
        value_block = lax.dynamic_slice_in_dim(
            back_value_piece, step_index * back_step_rows, back_step_rows, 0
        )
        prob_low, grad_raw, k_rel = block_grads(
            content_heads,
            q_rel,
            item_of,
            frame_index,
            grad_out_heads,
            log_total,
            delta_rows,
            key_block,
            value_block,
            step_index * back_step_rows,
            stream_lengths,
        )
        grad_content = grad_content + jnp.einsum(
            "hqk,khe->qhe",
            grad_raw,
            key_block.reshape(back_step_rows, HEADS, HEAD),
            preferred_element_type=jnp.float32,
        )
        grad_rel = grad_rel + jnp.einsum(
            "hqk,kc->qhc", grad_raw, k_rel, preferred_element_type=jnp.float32
        )
        key_part = jnp.einsum(
            "hqk,qhe->khe", grad_raw, content_heads, preferred_element_type=jnp.float32
        ).reshape(back_step_rows, D)
        value_part = jnp.einsum(
            "hqk,qhe->khe", prob_low, grad_out_heads, preferred_element_type=jnp.float32
        ).reshape(back_step_rows, D)
        return ((grad_content, grad_rel), (key_part, value_part))

    inner_state, block_parts = lax.scan(
        back_one_step,
        (back_start_state[0], back_start_state[1]),
        jnp.arange(extent // back_step_rows, dtype=jnp.int32),
    )
    key_all = block_parts[0].reshape(extent, D)
    value_all = block_parts[1].reshape(extent, D)
    grad_content, grad_rel, key_all, value_all = (
        inner_state[0],
        inner_state[1],
        key_all,
        value_all,
    )
    grad_keys, grad_values = (
        lax.psum_scatter(key_all, "tm", scatter_dimension=0, tiled=True),
        lax.psum_scatter(value_all, "tm", scatter_dimension=0, tiled=True),
    )
    half_size = D // 2
    rel_first = grad_rel[..., :half_size]
    rel_second = grad_rel[..., half_size:]
    sine_wide = sine_rows[:, None, :]
    cosine_wide = cosine_rows[:, None, :]
    grad_projected = jnp.concatenate(
        [
            rel_first * sine_wide - rel_second * cosine_wide,
            rel_first * cosine_wide + rel_second * sine_wide,
        ],
        axis=-1,
    ).astype(jnp.bfloat16)
    grad_pos_weight = jnp.einsum(
        "thc,the->che", grad_projected, position_heads, preferred_element_type=jnp.float32
    ).reshape(D, D)
    grad_q_position = jnp.einsum(
        "thc,che->the", grad_projected, pos_heads, preferred_element_type=jnp.float32
    )
    grad_content_bias = jnp.sum(grad_content, axis=0).reshape(D)
    grad_position_bias = jnp.sum(grad_q_position, axis=0).reshape(D)
    grad_query = (grad_content + grad_q_position).reshape(row_count, D).astype(jnp.bfloat16)
    grad_qkv = jnp.concatenate(
        [grad_query, grad_keys.astype(jnp.bfloat16), grad_values.astype(jnp.bfloat16)], axis=1
    )
    grad_qkv_weight = jnp.einsum(
        "tc,tf->cf", attn_norm_low, grad_qkv, preferred_element_type=jnp.float32
    )
    grad_attn_norm = jnp.einsum(
        "tf,cf->tc", grad_qkv, qkv_weight, preferred_element_type=jnp.float32
    )
    grad_from_attn, grad_ln_attn_gain, grad_ln_attn_bias = attn_pull(grad_attn_norm)
    grad_from_mlp, grad_ln_mlp_gain, grad_ln_mlp_bias = mlp_pull(grad_mlp_norm)
    grad_inputs = grad_rows + grad_from_attn + grad_from_mlp
    weight_grads = (
        grad_ln_attn_gain,
        grad_ln_attn_bias,
        grad_ln_mlp_gain,
        grad_ln_mlp_bias,
        grad_qkv_weight,
        grad_content_bias,
        grad_position_bias,
        grad_pos_weight,
        grad_out_weight,
        grad_up_weight,
        grad_up_bias,
        grad_gate_norm_gain,
        grad_gate_norm_bias,
        grad_conv_kernel,
        grad_conv_bias,
        grad_down_weight,
        grad_down_bias,
        grad_merge_weight,
        grad_merge_bias,
    )
    summed = lax.psum(
        (
            weight_grads[0],
            weight_grads[1],
            weight_grads[2],
            weight_grads[3],
            weight_grads[4],
            weight_grads[5],
            weight_grads[6],
            weight_grads[7],
            weight_grads[8],
            weight_grads[9],
            weight_grads[10],
            weight_grads[11],
            weight_grads[12],
            weight_grads[13],
            weight_grads[14],
            weight_grads[15],
            weight_grads[16],
            weight_grads[17],
            weight_grads[18],
        ),
        "tm",
    )
    shares = (
        lax.psum_scatter(
            summed[0].astype(jnp.bfloat16), "stream", scatter_dimension=0, tiled=True
        ).astype(jnp.float32),
        lax.psum_scatter(
            summed[1].astype(jnp.bfloat16), "stream", scatter_dimension=0, tiled=True
        ).astype(jnp.float32),
        lax.psum_scatter(
            summed[2].astype(jnp.bfloat16), "stream", scatter_dimension=0, tiled=True
        ).astype(jnp.float32),
        lax.psum_scatter(
            summed[3].astype(jnp.bfloat16), "stream", scatter_dimension=0, tiled=True
        ).astype(jnp.float32),
        lax.psum_scatter(
            summed[4].astype(jnp.bfloat16), "stream", scatter_dimension=0, tiled=True
        ).astype(jnp.float32),
        lax.psum_scatter(
            summed[5].astype(jnp.bfloat16), "stream", scatter_dimension=0, tiled=True
        ).astype(jnp.float32),
        lax.psum_scatter(
            summed[6].astype(jnp.bfloat16), "stream", scatter_dimension=0, tiled=True
        ).astype(jnp.float32),
        lax.psum_scatter(
            summed[7].astype(jnp.bfloat16), "stream", scatter_dimension=0, tiled=True
        ).astype(jnp.float32),
        lax.psum_scatter(
            summed[8].astype(jnp.bfloat16), "stream", scatter_dimension=0, tiled=True
        ).astype(jnp.float32),
        lax.psum_scatter(
            summed[9].astype(jnp.bfloat16), "stream", scatter_dimension=0, tiled=True
        ).astype(jnp.float32),
        lax.psum_scatter(
            summed[10].astype(jnp.bfloat16), "stream", scatter_dimension=0, tiled=True
        ).astype(jnp.float32),
        lax.psum_scatter(
            summed[11].astype(jnp.bfloat16), "stream", scatter_dimension=0, tiled=True
        ).astype(jnp.float32),
        lax.psum_scatter(
            summed[12].astype(jnp.bfloat16), "stream", scatter_dimension=0, tiled=True
        ).astype(jnp.float32),
        lax.psum_scatter(
            summed[13].astype(jnp.bfloat16), "stream", scatter_dimension=1, tiled=True
        ).astype(jnp.float32),
        lax.psum_scatter(
            summed[14].astype(jnp.bfloat16), "stream", scatter_dimension=0, tiled=True
        ).astype(jnp.float32),
        lax.psum_scatter(
            summed[15].astype(jnp.bfloat16), "stream", scatter_dimension=0, tiled=True
        ).astype(jnp.float32),
        lax.psum_scatter(
            summed[16].astype(jnp.bfloat16), "stream", scatter_dimension=0, tiled=True
        ).astype(jnp.float32),
        lax.psum_scatter(
            summed[17].astype(jnp.bfloat16), "stream", scatter_dimension=0, tiled=True
        ).astype(jnp.float32),
        lax.psum_scatter(
            summed[18].astype(jnp.bfloat16), "stream", scatter_dimension=0, tiled=True
        ).astype(jnp.float32),
    )
    return (out_rows, grad_inputs[None]) + tuple(shares)


LANES = 128
LOW = LANES // 2
BLOCK = 128
TALL = 256
WINDOW = 64
MARGIN = 16
BOUNDS = 16
MEGA = 1024 * 1024
RATE = 1150000000
F32 = jnp.float32
BF16 = jnp.bfloat16


def dot_nn(left, right):
    return jnp.dot(left, right, preferred_element_type=F32)


def dot_nt(left, right):
    return lax.dot_general(left, right, (((1,), (1,)), ((), ())), preferred_element_type=F32)


def dot_tn(left, right):
    return lax.dot_general(left, right, (((0,), (0,)), ((), ())), preferred_element_type=F32)


def rows_of(index, size, base=0):
    return pl.ds(pl.multiple_of(index * size, size) + base, size)


def line_of(ref):
    return ref[...].astype(F32).reshape(1, ref.shape[0])


def fold_rows(values):
    return jnp.sum(values.reshape(values.shape[0] // 8, 8, values.shape[1]), axis=0)


def one_row(values):
    return jnp.sum(values, axis=0, keepdims=True)


def turn(values):
    return pltpu.roll(values, LOW, 1)


def low_lanes(rows):
    return lax.broadcasted_iota(jnp.int32, (rows, LANES), 1) < LOW


def centre_rows(inputs):
    mean = jnp.mean(inputs, axis=-1, keepdims=True)
    centred = inputs - mean
    spread = jnp.mean(centred * centred, axis=-1, keepdims=True)
    return centred * lax.rsqrt(spread + EPS)


ERF_SCALE = 0.3275911 / math.sqrt(2.0)
ERF_TERMS = tuple(0.5 * term for term in (1.061405429, -1.453152027, 1.421413741, -0.284496736, 0.254829592))


def gelu_parts(values):
    bell = jnp.exp(values * values * -0.5)
    size = 1.0 + ERF_SCALE * jnp.abs(values)
    place = pl.reciprocal(size, approx=True)
    place = place * (2.0 - size * place)
    series = ERF_TERMS[0]
    for term in ERF_TERMS[1:]:
        series = series * place + term
    tail = series * place * bell
    phi = jnp.where(values < 0.0, tail, 1.0 - tail)
    return values * phi, phi + values * bell * (1.0 / math.sqrt(2.0 * math.pi))


class Part:
    def __init__(self, shape=None, pairs=None, refs=1):
        self.shape, self.pairs, self.refs = shape, pairs, refs

    def buffer(self, operand):
        return self.shape or operand.shape

    def copies(self, refs, buffer):
        return self.pairs(refs, buffer) if self.pairs else [(refs[0], buffer)]


def blocks_part(lanes):
    def pairs(refs, buffer):
        place = lax.axis_index("tm")
        return [
            (
                ref.at[:, pl.ds(lanes[0], lanes[1])],
                buffer.at[rows_of(lax.bitwise_xor(jnp.int32(apart), place), BLOCK)],
            )
            for apart, ref in enumerate(refs)
        ]

    return Part((HEADS * BLOCK, lanes[1]), pairs, HEADS)


def rows_part(first, size):
    return Part((size, D), lambda refs, buffer: [(refs[0].at[pl.ds(first, size)], buffer)])


class Fetch:
    def __init__(self, pairs, buffer, sems, first):
        self.buffer = buffer
        self.pending = [
            pltpu.make_async_copy(source, target, sems.at[first + index])
            for index, (source, target) in enumerate(pairs)
        ]
        for copy in self.pending:
            copy.start()

    def __call__(self):
        for copy in self.pending:
            copy.wait()
        self.pending = []
        return self.buffer


class Send:
    def __init__(self, buffer, target, sem):
        self.buffer, self.copy, self.begun = buffer, pltpu.make_async_copy(buffer, target, sem), False

    def go(self):
        if not self.begun:
            self.copy.start()
        self.begun = True


SPACES = {"v": pltpu.VMEM, "s": pltpu.SMEM}


def kernel_call(body, out_shapes, plan, scratch=(), micros=2, megas=58, bounds=False):
    def call(*operands):
        in_specs, buffers, at = [], [], 0
        for item in plan:
            if isinstance(item, Part):
                in_specs += [pl.BlockSpec(memory_space=pl.ANY)] * item.refs
                buffers.append(pltpu.VMEM(item.buffer(operands[at]), operands[at].dtype))
                at += item.refs
            else:
                in_specs.append(pl.BlockSpec(memory_space=SPACES[item]))
                at += 1
        sent = [out for out in out_shapes if len(out) > 2]
        buffers += [pltpu.VMEM(out[0], out[1]) for out in sent]
        sem_count = 64
        extra = [pltpu.SMEM((BOUNDS,), jnp.int32)] if bounds else []

        def outer(*refs):
            inputs, rest = refs[: len(in_specs)], refs[len(in_specs) :]
            outputs, rest = rest[: len(out_shapes)], rest[len(out_shapes) :]
            held, rest = list(rest[: len(buffers)]), rest[len(buffers) :]
            sems, rest = rest[0], rest[1:]
            given, at, used = [], 0, 0
            for item in plan:
                if isinstance(item, Part):
                    buffer = held.pop(0)
                    pairs = item.copies(inputs[at : at + item.refs], buffer)
                    given.append(Fetch(pairs, buffer, sems, used))
                    used += len(pairs)
                    at += item.refs
                else:
                    given.append(inputs[at])
                    at += 1
            results = []
            for out, ref in zip(out_shapes, outputs):
                if len(out) > 2:
                    results.append(Send(held.pop(0), ref, sems.at[used]))
                    used += 1
                else:
                    results.append(ref)
            assert used <= sem_count
            body(*given, *results, *rest)
            for item in given:
                if isinstance(item, Fetch):
                    item()
            sends = [item for item in results if isinstance(item, Send)]
            for item in sends:
                item.go()
            for item in sends:
                item.copy.wait()

        return pl.pallas_call(
            outer,
            out_shape=[jax.ShapeDtypeStruct(out[0], out[1]) for out in out_shapes],
            in_specs=in_specs,
            out_specs=[pl.BlockSpec(memory_space=pl.ANY if len(out) > 2 else pltpu.VMEM) for out in out_shapes],
            scratch_shapes=buffers
            + [pltpu.SemaphoreType.DMA((sem_count,))]
            + [pltpu.VMEM(shape, kind) for shape, kind in scratch]
            + extra,
            compiler_params=pltpu.CompilerParams(vmem_limit_bytes=megas * MEGA),
            cost_estimate=pl.CostEstimate(flops=micros * RATE, bytes_accessed=1 << 20, transcendentals=0),
        )(*operands)

    return call


def fill_bounds(lengths_ref, bounds_s, total):
    bounds_s[0] = jnp.int32(0)
    end = jnp.int32(0)
    for item in range(ITEMS):
        end = end + lengths_ref[0, item]
        bounds_s[item + 1] = end
    for item in range(ITEMS + 1, BOUNDS):
        bounds_s[item] = jnp.int32(total)


def stats_kernel(x_ref, cot_ref, gain_ref, bias_ref, up_ref, up_bias_ref, out_ref, pre_s):
    normed = centre_rows(x_ref[...].astype(F32)) * line_of(gain_ref) + line_of(bias_ref)
    pre_s[...] = dot_nn(normed.astype(BF16), up_ref()[...])
    out_ref[:, :D] = cot_ref[...]
    up_bias = line_of(up_bias_ref)[:, HALF:]

    @pl.loop(0, x_ref.shape[0] // 16, unroll=2)
    def _(step):
        rows = rows_of(step, 16)
        hidden, _ = gelu_parts(pre_s[rows] + up_bias)
        mean = jnp.mean(hidden, axis=-1, keepdims=True)
        centred = hidden - mean
        rate = lax.rsqrt(jnp.mean(centred * centred, axis=-1, keepdims=True) + EPS)
        lane = lax.broadcasted_iota(jnp.int32, (16, LANES), 1)
        mean_high = mean.astype(BF16).astype(F32)
        rate_high = rate.astype(BF16).astype(F32)
        packed = jnp.where(lane == 0, mean_high, mean - mean_high)
        packed = jnp.where(lane == 2, rate_high, packed)
        packed = jnp.where(lane == 3, rate - rate_high, packed)
        out_ref[rows, D:] = packed.astype(BF16)


def select_kernel(
    up_ref,
    up_bias_ref,
    gain_ref,
    bias_ref,
    conv_bias_ref,
    taps_ref,
    qkv_ref,
    pos_ref,
    content_ref,
    position_ref,
    up_out,
    table_out,
    qkv_out,
    pos_out,
    bias_out,
):
    place = lax.axis_index("tm")
    quarters = lax.axis_size("stream")
    share = HALF // (quarters * lax.axis_size("tm"))
    lane = lax.broadcasted_iota(jnp.int32, (1, 2 * LANES), 1)
    channel = jnp.where(lane < LANES + LOW, lane, lane - LOW)
    group = jnp.zeros_like(channel)
    for quarter in range(1, quarters):
        group = group + (channel >= quarter * share).astype(jnp.int32)
    source = group * (HALF // quarters) + share * place + channel - group * share
    chosen = (lax.broadcasted_iota(jnp.int32, (HALF, 2 * LANES), 0) == source).astype(F32).astype(BF16)
    gate = dot_nn(up_ref[:, :HALF], chosen)
    conv = dot_nn(up_ref[:, HALF:], chosen)
    up_out[:, :LANES] = gate[:, :LANES].astype(BF16)
    up_out[:, LANES : 2 * LANES] = jnp.where(low_lanes(D), gate[:, LANES:], conv[:, LANES:]).astype(BF16)
    up_out[:, 2 * LANES :] = conv[:, :LANES].astype(BF16)
    up_bias = line_of(up_bias_ref)
    lines = jnp.concatenate(
        [
            up_bias[:, :HALF],
            up_bias[:, HALF:],
            line_of(gain_ref),
            line_of(bias_ref),
            line_of(conv_bias_ref),
            jnp.zeros((3, HALF), F32),
        ],
        axis=0,
    )
    lines = dot_nn(lines.astype(BF16), chosen)
    taps = dot_nn(taps_ref[...], chosen)
    for part in range(2):
        lanes = slice(part * LANES, (part + 1) * LANES)
        table_out[part, :8] = lines[:, lanes]
        table_out[part, 8 : 8 + KERNEL] = taps[:, lanes]
        table_out[part, 8 + KERNEL :] = jnp.zeros((1, LANES), F32)

    odd = lax.rem(place, 2) == 1

    def head_lanes(ref, base):
        at = pl.ds(pl.multiple_of(lax.div(place, 2) * LANES + base, LANES), LANES)
        values = ref[:, at].astype(F32)
        values = jnp.where(odd, turn(values), values)
        return jnp.where(low_lanes(values.shape[0]), values, 0.0)

    for part in range(3):
        qkv_out[:, part * LANES : (part + 1) * LANES] = head_lanes(qkv_ref, part * D).astype(BF16)
    pos_out[...] = head_lanes(pos_ref, 0).astype(BF16)
    bias_out[...] = jnp.zeros((8, LANES), F32)
    for line, ref in enumerate((content_ref, position_ref)):
        values = line_of(ref)
        picked = values[:, :LANES]
        for tile in range(1, D // LANES):
            picked = jnp.where(
                lax.div(place, 2) == tile, values[:, tile * LANES : (tile + 1) * LANES], picked
            )
        picked = jnp.where(odd, turn(picked), picked)
        bias_out[line : line + 1] = jnp.where(low_lanes(1), picked, 0.0)


def angle_rows(coarse_ref, fine_ref, block, rows):
    half = D // 2
    base = coarse_ref[pl.ds(block, 1)]
    base_sine, base_cosine = base[:, :half], base[:, half:]
    sine, cosine = fine_ref[rows, :half], fine_ref[rows, half:]
    return base_sine * cosine + base_cosine * sine, base_cosine * cosine - base_sine * sine


def item_codes(bounds_s, index):
    code = jnp.zeros_like(index)
    for item in range(1, ITEMS + 1):
        code = code + (index >= bounds_s[item]).astype(jnp.int32)
    return jnp.where(code < ITEMS, code, ITEMS + index)


def attend_kernel(
    lengths_ref,
    x_ref,
    attn_gain_ref,
    attn_bias_ref,
    mlp_gain_ref,
    mlp_bias_ref,
    qkv_ref,
    pos_ref,
    bias_ref,
    coarse_ref,
    fine_ref,
    n_attn_out,
    n_mlp_out,
    hat_out,
    q_position_out,
    query_out,
    key_out,
    value_out,
    prob_out,
    attn_out,
    share_out,
    bounds_s,
):
    frames = n_attn_out.buffer.shape[0]
    half = D // 2
    fill_bounds(lengths_ref, bounds_s, frames)
    attn_gain, attn_bias = line_of(attn_gain_ref), line_of(attn_bias_ref)
    mlp_gain, mlp_bias = line_of(mlp_gain_ref), line_of(mlp_bias_ref)
    content, position = bias_ref[0:1], bias_ref[1:2]
    x_ref = x_ref()

    @pl.loop(0, frames // TALL, unroll=2)
    def _(block):
        rows = rows_of(block, TALL)
        for part in range(TALL // 32):
            at = rows_of(block, TALL, part * 32)
            at = pl.ds(pl.multiple_of(block * TALL + part * 32, 32), 32)
            hat = centre_rows(x_ref[at].astype(F32))
            hat_out.buffer[at] = hat.astype(BF16)
            n_attn_out.buffer[at] = (hat * attn_gain + attn_bias).astype(BF16)
            n_mlp_out.buffer[at] = (hat * mlp_gain + mlp_bias).astype(BF16)
        parts = dot_nn(n_attn_out.buffer[rows], qkv_ref[...])
        query = parts[:, :LANES]
        query_out.buffer[rows, :LANES] = ((query + content).astype(BF16).astype(F32) * 0.125).astype(BF16)
        q_position = (query + position).astype(BF16)
        q_position_out.buffer[rows] = q_position
        key_out.buffer[rows, :LANES] = parts[:, LANES : 2 * LANES].astype(BF16)
        value_out.buffer[rows] = parts[:, 2 * LANES :].astype(BF16)
        projected = dot_nt(q_position, pos_ref[...])
        for part in range(TALL // 32):
            at = pl.ds(pl.multiple_of(block * TALL + part * 32, 32), 32)
            inner = part * 32 % BLOCK
            sine, cosine = angle_rows(
                coarse_ref, fine_ref, block * (TALL // BLOCK) + part * 32 // BLOCK, slice(inner, inner + 32)
            )
            first = projected[part * 32 : part * 32 + 32, :half]
            second = projected[part * 32 : part * 32 + 32, half:]
            query_out.buffer[at, LANES : LANES + half] = ((first * sine + second * cosine) * 0.125).astype(BF16)
            query_out.buffer[at, LANES + half :] = ((second * sine - first * cosine) * 0.125).astype(BF16)
            key_out.buffer[at, LANES : LANES + half] = cosine.astype(BF16)
            key_out.buffer[at, LANES + half :] = sine.astype(BF16)

    for out in (n_attn_out, n_mlp_out, hat_out, q_position_out, query_out, key_out, value_out):
        out.go()
    key_code = item_codes(bounds_s, lax.broadcasted_iota(jnp.int32, (1, frames), 1))

    @pl.loop(0, frames // TALL, unroll=2)
    def _(block):
        rows = rows_of(block, TALL)
        raw = dot_nt(query_out.buffer[rows], key_out.buffer[...])
        for part in range(TALL // 32):
            start = block * TALL + part * 32
            at = pl.ds(pl.multiple_of(start, 32), 32)
            index = start + lax.broadcasted_iota(jnp.int32, (32, 1), 0)
            scaled = jnp.where(
                item_codes(bounds_s, index) == key_code, raw[part * 32 : part * 32 + 32], MASKED
            )
            weight = jnp.exp(scaled - jnp.max(scaled, axis=1, keepdims=True))
            prob_out.buffer[at] = weight.astype(BF16)
            share_out.buffer[at] = jnp.broadcast_to(1.0 / jnp.sum(weight, axis=1, keepdims=True), (32, LANES))
        attn_out.buffer[rows] = (
            dot_nn(prob_out.buffer[rows], value_out.buffer[...]) * share_out.buffer[rows]
        )


def fill_margins(wide_s, frames):
    edge = jnp.zeros((MARGIN, LANES), F32)
    wide_s[:MARGIN] = edge
    wide_s[MARGIN + frames : 2 * MARGIN + frames] = edge
    base = frames + 3 * MARGIN
    after = base + frames // 2
    low = low_lanes(MARGIN)
    wide_s[base - MARGIN : base] = jnp.where(low, 0.0, turn(wide_s[after - MARGIN : after]))
    wide_s[after : after + MARGIN] = jnp.where(low, turn(wide_s[base : base + MARGIN]), 0.0)


def item_span(bounds_s, frame):
    begin, end = bounds_s[0], bounds_s[BOUNDS - 1]
    for item in range(1, ITEMS + 1):
        edge = bounds_s[item]
        begin = jnp.where(frame >= edge, edge, begin)
    for item in range(ITEMS, 0, -1):
        edge = bounds_s[item]
        end = jnp.where(frame < edge, edge, end)
    return begin, end


def is_whole(bounds_s, start):
    begin, end = item_span(bounds_s, start)
    reach = KERNEL // 2
    low = (begin == 0) | (begin <= start - reach)
    high = (end == bounds_s[BOUNDS - 1]) | (end >= start + WINDOW + reach)
    return low & high & (end >= start + WINDOW)


def tap_limits(bounds_s, start):
    frame = start + lax.broadcasted_iota(jnp.int32, (WINDOW, LANES), 0)
    begin, end = item_span(bounds_s, frame)
    return begin - frame, end - frame


def grouped(values):
    return values.reshape(WINDOW // 8, 8, LANES)


def triple_places(step, frames):
    half = frames // 2
    return (
        pl.multiple_of(step * WINDOW, 2 * MARGIN),
        pl.multiple_of(step * WINDOW + half, 2 * MARGIN),
        pl.multiple_of(step * WINDOW + frames + 2 * MARGIN, 2 * MARGIN),
    )


def over_windows(bounds_s, frames, body):
    half = frames // 2

    @pl.loop(0, half // WINDOW)
    def _(step):
        start = step * WINDOW
        whole = is_whole(bounds_s, start) & is_whole(bounds_s, start + half)

        @pl.when(whole)
        def _():
            body(step, None)

        @pl.when(jnp.logical_not(whole))
        def _():
            first, second = tap_limits(bounds_s, start), tap_limits(bounds_s, start + half)
            low = low_lanes(WINDOW)
            rest = [jnp.where(low, one, other) for one, other in zip(first, second)]
            body(step, (first, second, rest))


def tap_view(window_ref, tap, limits):
    view = window_ref[tap + 1 : tap + 1 + WINDOW]
    if limits is not None:
        shift = tap - KERNEL // 2
        view = jnp.where((limits[0] <= shift) & (limits[1] > shift), view, 0.0)
    return grouped(view)


def mlp_first_kernel(
    lengths_ref,
    n_ref,
    up_ref,
    table_ref,
    stats_ref,
    cot_ref,
    merge_ref,
    down_ref,
    attn_ref,
    mixed_out,
    gate_pre_out,
    gy_out,
    hat_out,
    slope_out,
    down_out,
    vectors_out,
    lines_out,
    hidden_s,
    gate_slope_s,
    conv_s,
    grad_s,
    out_s,
    back_s,
    branch_s,
    mix_s,
    taps_s,
    turn_s,
    tap_sum_s,
    columns_s,
    forward_s,
    backward_s,
    bounds_s,
):
    frames = mix_s.shape[0]
    half = frames // 2
    blocks = frames // BLOCK
    quarters, down_rows, _ = down_out.shape
    share = down_rows // 4
    channels = quarters * share
    fill_bounds(lengths_ref, bounds_s, frames)
    for part in range(2):
        for tap in range(KERNEL):
            line = jnp.broadcast_to(table_ref[part, 8 + tap : 9 + tap], (8, LANES))
            taps_s[part, tap] = line
            turn_s[part, KERNEL - 1 - tap] = line
    tap_sum_s[...] = jnp.zeros(tap_sum_s.shape, F32)
    main, rest = table_ref[0, :8], table_ref[1, :8]
    mixed_bias = jnp.where(low_lanes(1), rest[0:1], rest[1:2])
    low = low_lanes(64)
    hat_ref, slope_ref, gy_ref, gate_pre_ref = hat_out.buffer, slope_out.buffer, gy_out.buffer, gate_pre_out.buffer
    n_ref = n_ref()
    stats_ref = stats_ref()

    def stat_rows(rows):
        stats = stats_ref[rows].astype(F32)
        return stats[:, 0:1] + stats[:, 1:2], stats[:, 2:3] + stats[:, 3:4]

    def chunk(start, base=0):
        return pl.ds(pl.multiple_of(start, 64) + base, 64)

    def conv_part(hidden, mean, rate, lines, rows, to_rows):
        hat = (hidden - mean) * rate
        hat_ref[rows] = hat
        conv_s[to_rows] = (hat * lines[2:3] + lines[3:4]).astype(BF16).astype(F32)

    @pl.loop(0, half // TALL)
    def _(block):
        pre = [dot_nn(n_ref[rows_of(block, TALL, base)], up_ref[...]) for base in (0, half)]
        for part in range(TALL // 64):
            inner = slice(part * 64, part * 64 + 64)
            start = block * TALL + part * 64
            mixed = []
            for values, base in zip(pre, (0, half)):
                rows = chunk(start, base)
                gate, gate_slope = gelu_parts(values[inner, :LANES] + main[0:1])
                hidden_s[rows] = gate
                gate_slope_s[rows] = gate_slope
                hidden, slope = gelu_parts(values[inner, 2 * LANES :] + main[1:2])
                slope_ref[rows] = slope
                mean, rate = stat_rows(rows)
                conv_part(hidden, mean, rate, main, rows, chunk(start, base + MARGIN))
                mixed.append((*gelu_parts(values[inner, LANES : 2 * LANES] + mixed_bias), mean, rate))
            (low_hidden, low_slope, low_mean, low_rate), (high_hidden, high_slope, high_mean, high_rate) = mixed
            rows = chunk(start, frames)
            hidden_s[rows] = jnp.where(low, low_hidden, turn(high_hidden))
            gate_slope_s[rows] = jnp.where(low, low_slope, turn(high_slope))
            slope_ref[rows] = jnp.where(low, turn(low_slope), high_slope)
            conv_part(
                jnp.where(low, turn(low_hidden), high_hidden),
                jnp.where(low, low_mean, high_mean),
                jnp.where(low, low_rate, high_rate),
                rest,
                rows,
                chunk(start, frames + 3 * MARGIN),
            )

    hat_out.go()
    slope_out.go()
    fill_margins(conv_s, frames)
    tall = WINDOW + 2 * MARGIN
    outs = (0, half, frames)

    def convolve(step, limits):
        for index, base in enumerate(triple_places(step, frames)):
            forward_s[index] = conv_s[pl.ds(base, tall)]
        for index in range(3):
            own = None if limits is None else limits[index]
            total = jnp.zeros((WINDOW // 8, 8, LANES), F32)
            for tap in range(KERNEL):
                total = total + tap_view(forward_s.at[index], tap, own) * taps_s[index // 2, tap][None]
            lines = rest if index == 2 else main
            out_s[rows_of(step, WINDOW, outs[index])] = total.reshape(WINDOW, LANES) + lines[4:5]

    over_windows(bounds_s, frames, convolve)
    cot_ref = cot_ref()
    merge_ref = merge_ref()
    down_ref = down_ref()
    attn_ref = attn_ref()
    down_ref[channels:] = jnp.zeros((2 * LANES - channels, D), BF16)
    zero = jnp.zeros((8, LANES), F32)

    def branch_part(grad_gated, rows, to_rows, sums):
        up_sum, conv_sum = sums
        gate, conv = hidden_s[rows], out_s[rows]
        gate_pre = (grad_gated * conv * gate_slope_s[rows]).astype(BF16)
        gate_pre_ref[rows] = gate_pre
        grad_conv = (grad_gated * gate).astype(BF16).astype(F32)
        grad_s[to_rows] = grad_conv
        return gate * conv, (up_sum + fold_rows(gate_pre.astype(F32)), conv_sum + fold_rows(grad_conv))

    def branch_step(block, sums):
        main_sums, rest_sums = sums
        grads = []
        for base in (0, half):
            rows = rows_of(block, TALL, base)
            branch = dot_nt(cot_ref[rows], merge_ref[...]).astype(BF16)
            branch_s[rows] = branch
            grads.append(dot_nt(branch, down_ref[...]))
        for part in range(TALL // 64):
            inner = slice(part * 64, part * 64 + 64)
            start = block * TALL + part * 64
            for values, base in zip(grads, (0, half)):
                rows = chunk(start, base)
                gated, main_sums = branch_part(
                    values[inner, :LANES], rows, chunk(start, base + MARGIN), main_sums
                )
                mix_s[rows, :LANES] = gated.astype(BF16)
            grad = jnp.where(low, grads[0][inner, LANES:], turn(grads[1][inner, LANES:]))
            gated, rest_sums = branch_part(
                grad, chunk(start, frames), chunk(start, frames + 3 * MARGIN), rest_sums
            )
            low_rows, high_rows = chunk(start), chunk(start, half)
            mix_s[low_rows, LANES:] = jnp.where(low, gated, turn(attn_ref[low_rows])).astype(BF16)
            mix_s[high_rows, LANES:] = jnp.where(low, turn(gated), turn(attn_ref[high_rows])).astype(BF16)
        return main_sums, rest_sums

    (main_up, main_conv), (rest_up, rest_conv) = lax.fori_loop(
        0, half // TALL, branch_step, ((zero, zero), (zero, zero))
    )
    gate_pre_out.go()
    fill_margins(grad_s, frames)
    ones = jnp.ones((16, frames), BF16)
    lines_out[0:1] = dot_nn(ones, branch_s[...])[0:1]
    lines_out[1:2] = dot_nn(ones, cot_ref[...])[0:1]
    lines_out[2:8] = jnp.zeros((6, D), F32)
    grad_down = dot_tn(mix_s[...], branch_s[...])
    for quarter in range(quarters):
        for tile in range(4):
            down_out[quarter, tile * share : (tile + 1) * share] = grad_down[
                quarter * share : (quarter + 1) * share, tile * LANES : (tile + 1) * LANES
            ].astype(BF16)

    def differentiate(step, limits):
        for index, base in enumerate(triple_places(step, frames)):
            forward_s[index] = conv_s[pl.ds(base, tall)]
            backward_s[index] = grad_s[pl.ds(base, tall)]
        for index in range(3):
            own = None if limits is None else limits[index]
            total = jnp.zeros((WINDOW // 8, 8, LANES), F32)
            centre = grouped(backward_s[index, MARGIN : MARGIN + WINDOW])
            for tap in range(KERNEL):
                total = total + tap_view(backward_s.at[index], tap, own) * turn_s[index // 2, tap][None]
                tap_sum_s[index // 2, tap] += jnp.sum(tap_view(forward_s.at[index], tap, own) * centre, axis=0)
            back_s[rows_of(step, WINDOW, outs[index])] = total.reshape(WINDOW, LANES)

    over_windows(bounds_s, frames, differentiate)
    lane = lax.broadcasted_iota(jnp.int32, (64, LANES), 1)

    def norm_part(rows, lines, sums):
        gain_sum, bias_sum = sums
        back, hat = back_s[rows], hat_ref[rows]
        grad = back * lines[2:3]
        gy_ref[rows] = grad
        along = back * hat
        return grad, along * lines[2:3], (gain_sum + fold_rows(along), bias_sum + fold_rows(back))

    def norm_step(block, sums):
        main_sums, rest_sums = sums
        for part in range(TALL // 64):
            start = block * TALL + part * 64
            pairs = []
            for base in (0, half):
                plain, along, main_sums = norm_part(chunk(start, base), main, main_sums)
                pairs.append([plain, along])
            plain, along, rest_sums = norm_part(chunk(start, frames), rest, rest_sums)
            for item, values in enumerate((plain, along)):
                pairs[0][item] = pairs[0][item] + jnp.where(low, values, 0.0)
                pairs[1][item] = pairs[1][item] + jnp.where(low, 0.0, values)
            for (plain, along), base in zip(pairs, (0, half)):
                columns_s[chunk(start, base)] = jnp.where(
                    lane == 0,
                    jnp.sum(plain, axis=-1, keepdims=True),
                    jnp.where(lane == 1, jnp.sum(along, axis=-1, keepdims=True), 0.0),
                )
        return main_sums, rest_sums

    (main_gain, main_bias), (rest_gain, rest_bias) = lax.fori_loop(
        0, half // TALL, norm_step, ((zero, zero), (zero, zero))
    )
    gy_out.go()
    totals = jnp.concatenate(
        [jnp.transpose(columns_s[block * BLOCK : (block + 1) * BLOCK])[:2] for block in range(blocks)], axis=0
    )
    high = totals.astype(BF16)
    low_part = (totals - high.astype(F32)).astype(BF16)
    for block in range(blocks):
        mixed_out[block, :BLOCK] = mix_s[block * BLOCK : (block + 1) * BLOCK]
        mixed_out[block, BLOCK:, :LANES] = high
        mixed_out[block, BLOCK:, LANES:] = low_part

    def vectors(part, lines):
        taps = jnp.sum(tap_sum_s[part], axis=1)[:KERNEL]
        stacked = jnp.concatenate([taps] + [one_row(line) for line in lines], axis=0)
        if part:
            stacked = stacked + turn(stacked)
        return jnp.transpose(
            jnp.concatenate([stacked, jnp.zeros((LANES - stacked.shape[0], LANES), F32)], axis=0)
        )

    vectors_out[:LANES] = vectors(0, (main_conv, main_gain, main_bias, main_up))
    vectors_out[LANES:] = vectors(1, (rest_conv, rest_gain, rest_bias, rest_up))[: channels - LANES]


def attend_back_kernel(
    cot_ref,
    merge_ref,
    head_ref,
    share_ref,
    value_ref,
    attn_ref,
    prob_ref,
    key_ref,
    coarse_ref,
    fine_ref,
    pos_ref,
    query_ref,
    n_ref,
    q_position_ref,
    qkv_ref,
    hat_ref,
    gain_ref,
    down_ref,
    branch_out,
    total_out,
    pack_0,
    pack_1,
    pack_2,
    pack_3,
    lines_out,
    grad_s,
    raw_s,
    projected_s,
    parts_s,
    grads_s,
):
    place = lax.axis_index("tm")
    stream = lax.axis_index("stream")
    frames = raw_s.shape[0]
    blocks = frames // BLOCK
    half = D // 2
    zero = jnp.zeros((8, LANES), F32)
    cot_ref, merge_ref, head_ref = cot_ref(), merge_ref(), head_ref()
    head_ref[HEAD:] = jnp.zeros((LANES - HEAD, D), BF16)
    share_ref, value_ref, attn_ref = share_ref(), value_ref(), attn_ref()
    prob_ref, key_ref, pos_ref = prob_ref(), key_ref(), pos_ref()

    def score_step(block, sums):
        content_sum, position_sum = sums
        rows = rows_of(block, TALL)
        branch = dot_nt(cot_ref[rows], merge_ref[...]).astype(BF16)
        branch_out.buffer[rows] = branch
        grad = (dot_nt(branch, head_ref[...]) * share_ref[rows]).astype(BF16)
        grad_s[rows] = grad
        score = dot_nt(grad, value_ref[...])
        for part in range(TALL // 32):
            at = pl.ds(pl.multiple_of(block * TALL + part * 32, 32), 32)
            inner = slice(part * 32, part * 32 + 32)
            delta = jnp.sum(grad[inner].astype(F32) * attn_ref[at], axis=1, keepdims=True)
            raw_s[at] = (prob_ref[at].astype(F32) * (score[inner] - delta)).astype(BF16)
        query = dot_nn(raw_s[rows], key_ref[...]) * 0.125
        for part in range(TALL // 32):
            at = pl.ds(pl.multiple_of(block * TALL + part * 32, 32), 32)
            inner = part * 32 % BLOCK
            sine, cosine = angle_rows(
                coarse_ref, fine_ref, block * (TALL // BLOCK) + part * 32 // BLOCK, slice(inner, inner + 32)
            )
            inner = slice(part * 32, part * 32 + 32)
            first, second = query[inner, LANES : LANES + half], query[inner, LANES + half :]
            projected_s[at, :half] = (first * sine - second * cosine).astype(BF16)
            projected_s[at, half:] = (first * cosine + second * sine).astype(BF16)
        position = dot_nn(projected_s[rows], pos_ref[...])
        content = query[:, :LANES]
        parts_s[rows, :LANES] = (content + position).astype(BF16)
        return content_sum + fold_rows(content), position_sum + fold_rows(position)

    content_sum, position_sum = lax.fori_loop(0, frames // TALL, score_step, (zero, zero), unroll=2)
    branch_out.go()
    query_ref, n_ref, q_position_ref = query_ref(), n_ref(), q_position_ref()
    qkv_ref, hat_ref = qkv_ref(), hat_ref()
    grad_key = dot_tn(query_ref[...], raw_s[...])
    grad_value = dot_tn(grad_s[...], prob_ref[...])
    for block in range(blocks):
        at = slice(block * BLOCK, (block + 1) * BLOCK)
        parts_s[at, LANES : 2 * LANES] = jnp.transpose(grad_key[:, at]).astype(BF16)
        parts_s[at, 2 * LANES :] = jnp.transpose(grad_value[:, at]).astype(BF16)
    grads_s[:HEAD] = dot_tn(parts_s[:, :LANES], n_ref[...])[:HEAD]
    grads_s[HEAD : 2 * HEAD] = dot_nn(grad_key.astype(BF16), n_ref[...])[:HEAD]
    grads_s[2 * HEAD : 3 * HEAD] = dot_nn(grad_value.astype(BF16), n_ref[...])[:HEAD]
    grads_s[3 * HEAD :] = dot_tn(q_position_ref[...], projected_s[...])[:HEAD]
    for apart, pack_out in enumerate((pack_0, pack_1, pack_2, pack_3)):
        quarter = lax.bitwise_xor(stream, jnp.int32(apart))
        lanes = pl.ds(pl.multiple_of(quarter * LANES, LANES), LANES)
        pack_out[: 4 * HEAD] = grads_s[:, lanes].astype(BF16)
        spare = 4 * HEAD + down_ref.shape[1]
        pack_out[4 * HEAD : spare] = down_ref[quarter]
        pack_out[spare:] = jnp.zeros((pack_out.shape[0] - spare, LANES), BF16)

    gain = line_of(gain_ref)
    wide_zero = jnp.zeros((8, D), F32)

    def norm_step(block, sums):
        gain_sum, bias_sum = sums
        grad = dot_nt(parts_s[rows_of(block, TALL)], qkv_ref[...])
        for part in range(TALL // 32):
            at = pl.ds(pl.multiple_of(block * TALL + part * 32, 32), 32)
            own = grad[part * 32 : part * 32 + 32]
            total_out.buffer[at] = (own * gain).astype(BF16)
            gain_sum = gain_sum + fold_rows(own * hat_ref[at].astype(F32))
            bias_sum = bias_sum + fold_rows(own)
        return gain_sum, bias_sum

    gain_sum, bias_sum = lax.fori_loop(0, frames // TALL, norm_step, (wide_zero, wide_zero), unroll=2)
    lane = lax.broadcasted_iota(jnp.int32, (1, LANES), 1)

    def own_lanes(sums):
        line = one_row(sums)
        line = line + turn(line)
        tiles = [
            jnp.where(lax.div(tile * LANES + lane, HEAD) == place, line, 0.0) for tile in range(D // LANES)
        ]
        return jnp.concatenate(tiles, axis=1)

    lines_out[...] = jnp.concatenate(
        [
            one_row(gain_sum),
            one_row(bias_sum),
            own_lanes(content_sum),
            own_lanes(position_sum),
            jnp.zeros((4, D), F32),
        ],
        axis=0,
    )


def mlp_second_kernel(
    mixed_ref,
    stats_ref,
    gate_pre_ref,
    gy_ref,
    hat_ref,
    slope_ref,
    up_ref,
    norm_hat_ref,
    gain_ref,
    other_ref,
    n_ref,
    vectors_ref,
    first_lines_ref,
    head_lines_ref,
    same_out,
    apart_out,
    pack_0,
    pack_1,
    pack_2,
    pack_3,
    pre_s,
    columns_s,
    grad_up_s,
    lines_s,
    up_columns_s,
):
    packs = (pack_0, pack_1, pack_2, pack_3)
    stream = lax.axis_index("stream")
    place = lax.axis_index("tm")
    frames = pre_s.shape[0]
    half = frames // 2
    blocks = frames // BLOCK
    quarters = len(packs)
    channels = vectors_ref.shape[0]
    share = channels // quarters
    totals = jnp.zeros((2 * blocks, LANES), F32)
    for source in range(mixed_ref.shape[0]):
        both = mixed_ref[source, BLOCK:].astype(F32)
        totals = totals + (both[:, :LANES] + both[:, LANES:])
    totals = totals * (1.0 / HALF)
    columns = jnp.transpose(jnp.concatenate([totals, jnp.zeros((LANES - 2 * blocks, LANES), F32)], axis=0))
    lane = lax.broadcasted_iota(jnp.int32, (BLOCK, LANES), 1)
    stats_ref = stats_ref()
    for block in range(blocks):
        at = slice(block * BLOCK, (block + 1) * BLOCK)
        stats = stats_ref[at].astype(F32)
        rate = stats[:, 2:3] + stats[:, 3:4]
        kept = jnp.where(lane == 0, columns[:, 2 * block : 2 * block + 1], rate)
        columns_s[at] = jnp.where(lane == 1, columns[:, 2 * block + 1 : 2 * block + 2], kept)
    gate_pre_ref, gy_ref, hat_ref, slope_ref = gate_pre_ref(), gy_ref(), hat_ref(), slope_ref()
    up_ref, norm_hat_ref, other_ref, n_ref = up_ref(), norm_hat_ref(), other_ref(), n_ref()
    low = low_lanes(64)
    gain = line_of(gain_ref)

    def chunk(start, base=0):
        return pl.ds(pl.multiple_of(start, 64) + base, 64)

    def pre_part(rows, table, up_sum):
        plain, along, rate = table
        grad = rate * (gy_ref[rows] - plain - hat_ref[rows] * along)
        pre = (grad * slope_ref[rows]).astype(BF16).astype(F32)
        return pre, up_sum + fold_rows(pre)

    def pre_step(block, sums):
        main_up, rest_up = sums
        for part in range(TALL // 64):
            start = block * TALL + part * 64
            tables = []
            for base in (0, half):
                rows = chunk(start, base)
                values = columns_s[rows]
                table = [values[:, item : item + 1] for item in range(3)]
                tables.append(table)
                pre, main_up = pre_part(rows, table, main_up)
                pre_s[rows, :LANES] = gate_pre_ref[rows]
                pre_s[rows, 2 * LANES :] = pre.astype(BF16)
            rows = chunk(start, frames)
            table = [jnp.where(low, one, other) for one, other in zip(*tables)]
            pre, rest_up = pre_part(rows, table, rest_up)
            gate_pre = gate_pre_ref[rows].astype(F32)
            pre_s[chunk(start), LANES : 2 * LANES] = jnp.where(low, gate_pre, turn(pre)).astype(BF16)
            pre_s[chunk(start, half), LANES : 2 * LANES] = jnp.where(low, turn(gate_pre), pre).astype(BF16)
        return main_up, rest_up

    zero = jnp.zeros((8, LANES), F32)
    main_up, rest_up = lax.fori_loop(0, half // TALL, pre_step, (zero, zero))
    grad_up_s[...] = dot_tn(pre_s[...], n_ref[...])
    wide_zero = jnp.zeros((8, D), F32)

    def norm_step(block, sums):
        gain_sum, bias_sum = sums
        rows = rows_of(block, BLOCK)
        grad = dot_nt(pre_s[rows], up_ref[...])
        total = (grad * gain + other_ref[rows].astype(F32)).astype(BF16)
        apart = lax.bitwise_xor(block, place)
        slot = lax.div(apart, 2)

        @pl.when(lax.rem(apart, 2) == 0)
        def _():
            same_out[slot] = total

        @pl.when(lax.rem(apart, 2) == 1)
        def _():
            apart_out[slot] = total

        return gain_sum + fold_rows(grad * norm_hat_ref[rows].astype(F32)), bias_sum + fold_rows(grad)

    gain_sum, bias_sum = lax.fori_loop(0, blocks, norm_step, (wide_zero, wide_zero))
    rest_line = one_row(rest_up)
    up_columns_s[:LANES] = jnp.transpose(jnp.broadcast_to(one_row(main_up), (LANES, LANES)))
    up_columns_s[LANES:] = jnp.transpose(jnp.broadcast_to(rest_line + turn(rest_line), (LANES, LANES)))[:LOW]
    first_device = (place == 0).astype(F32)
    lines_s[...] = jnp.concatenate(
        [
            head_lines_ref[0:2],
            one_row(gain_sum),
            one_row(bias_sum),
            head_lines_ref[2:4],
            first_lines_ref[0:2] * first_device,
            jnp.zeros((8, D), F32),
        ],
        axis=0,
    )
    gate_at = KERNEL + 3
    lane = lax.broadcasted_iota(jnp.int32, (share, LANES), 1)
    for apart, pack_out in enumerate(packs):
        quarter = lax.bitwise_xor(stream, jnp.int32(apart))
        lanes = pl.ds(pl.multiple_of(quarter * LANES, LANES), LANES)
        pack_out[:channels] = grad_up_s[:channels, lanes].astype(BF16)
        pack_out[channels : channels + LANES] = grad_up_s[2 * LANES :, lanes].astype(BF16)
        pack_out[channels + LANES : 2 * channels] = grad_up_s[channels : 2 * LANES, lanes].astype(BF16)
        table = vectors_ref[pl.ds(pl.multiple_of(quarter * share, 8), share)]
        for other in range(2):
            at = pl.ds(pl.multiple_of((2 * lax.rem(quarter, 2) + other) * share, 8), share)
            column = jnp.where(
                quarter < quarters // 2, vectors_ref[at][:, gate_at : gate_at + 1], up_columns_s[at][:, 0:1]
            )
            table = jnp.where(lane == gate_at + other, column, table)
        pack_out[2 * channels : 2 * channels + share] = table.astype(BF16)
        pack_out[2 * channels + share :] = lines_s[:, lanes].astype(BF16)


def output_kernel(
    x_ref, mixed_ref, head_ref, down_ref, down_bias_ref, merge_ref, merge_bias_ref, out_ref, joined_out
):
    sources = mixed_ref.shape[0]
    rows = x_ref.shape[0]
    channels = HALF // sources
    share = channels // 4
    attn_parts = []
    branch_attn = jnp.zeros((rows, D), F32)
    branch_mlp = jnp.zeros((rows, D), F32)
    for source in range(sources):
        attn = turn(mixed_ref[source, :rows, LANES:].astype(F32))[:, :HEAD].astype(BF16)
        attn_parts.append(attn)
        branch_attn = branch_attn + dot_nn(attn, head_ref[source * HEAD : (source + 1) * HEAD])
        down = jnp.concatenate(
            [down_ref[(part * sources + source) * share : (part * sources + source + 1) * share] for part in range(4)],
            axis=0,
        )
        branch_mlp = branch_mlp + dot_nn(mixed_ref[source, :rows, :channels], down)
    joined = jnp.concatenate(
        [branch_attn.astype(BF16), (branch_mlp + line_of(down_bias_ref)).astype(BF16)], axis=1
    )
    result = x_ref[...].astype(F32) + dot_nn(joined, merge_ref[...]) + line_of(merge_bias_ref)
    out_ref[...] = result.astype(BF16)
    turned = jnp.transpose(joined.astype(F32))
    heads = jnp.transpose(jnp.concatenate(attn_parts, axis=1).astype(F32))
    merge_share = turned.shape[0] // (4 * sources)
    head_share = heads.shape[0] // (4 * sources)
    used = 4 * (merge_share + head_share)
    for target in range(sources):
        for part in range(4):
            at = (part * sources + target) * merge_share
            joined_out[target, part * merge_share : (part + 1) * merge_share] = turned[
                at : at + merge_share
            ].astype(BF16)
            at = (part * sources + target) * head_share
            to = 4 * merge_share + part * head_share
            joined_out[target, to : to + head_share] = heads[at : at + head_share].astype(BF16)
        joined_out[target, used:] = jnp.zeros((joined_out.shape[1] - used, rows), BF16)


def merge_kernel(joined_ref, cot_ref, branch_ref, pack_0, pack_1, pack_2, pack_3, merge_s, head_s):
    stream = lax.axis_index("stream")
    sources, _, rows = joined_ref.shape
    merge_rows = 2 * D // sources
    head_rows = D // sources
    grad_merge = jnp.zeros((merge_rows, D), F32)
    grad_head = jnp.zeros((head_rows, D), F32)
    cot_ref, branch_ref = cot_ref(), branch_ref()
    for source in range(sources):
        at = slice(source * rows, (source + 1) * rows)
        grad_merge = grad_merge + dot_nn(joined_ref[source, :merge_rows], cot_ref[at])
        grad_head = grad_head + dot_nn(joined_ref[source, merge_rows : merge_rows + head_rows], branch_ref[at])
    merge_s[...] = grad_merge
    head_s[...] = grad_head
    for apart, pack_out in enumerate((pack_0, pack_1, pack_2, pack_3)):
        quarter = lax.bitwise_xor(stream, jnp.int32(apart))
        for grad_s, base in ((merge_s, 0), (head_s, merge_rows)):
            share = grad_s.shape[0] // 4
            at = pl.ds(pl.multiple_of(quarter * share, share), share)
            for tile in range(4):
                to = base + tile * share
                pack_out[to : to + share] = grad_s[at, tile * LANES : (tile + 1) * LANES].astype(BF16)


def pair_kernel(same_ref, other_ref, *out_refs):
    for slot, out_ref in enumerate(out_refs):
        out_ref[...] = (same_ref[slot].astype(F32) + other_ref[slot].astype(F32)).astype(BF16)


def frames_kernel(x_ref, cot_ref, *refs):
    total_refs, out_ref = refs[:-1], refs[-1]
    for part in range(x_ref.shape[0] // 32):
        rows = slice(part * 32, part * 32 + 32)
        inputs = x_ref[rows].astype(F32)
        mean = jnp.mean(inputs, axis=-1, keepdims=True)
        centred = inputs - mean
        rate = lax.rsqrt(jnp.mean(centred * centred, axis=-1, keepdims=True) + EPS)
        hat = centred * rate
        grad = total_refs[0][rows].astype(F32)
        for total_ref in total_refs[1:]:
            grad = grad + total_ref[rows].astype(F32)
        plain = jnp.mean(grad, axis=-1, keepdims=True)
        along = jnp.mean(grad * hat, axis=-1, keepdims=True)
        out_ref[rows] = cot_ref[rows].astype(F32) + rate * (grad - plain - hat * along)


def add_kernel(*refs):
    out_ref = refs[-1]
    first = 0
    for at in range(0, len(refs) - 1, 4):
        total = refs[at][...].astype(F32)
        for ref in refs[at + 1 : at + 4]:
            total = total + ref[...].astype(F32)
        out_ref[first : first + total.shape[0]] = total.astype(BF16)
        first += total.shape[0]


def early_kernel(all_ref, qkv_out, pos_out, down_out):
    sources = all_ref.shape[0]
    share = HALF // (4 * sources)
    for kind in range(4):
        lines = jnp.transpose(
            jnp.concatenate(
                [all_ref[source, kind * HEAD : (kind + 1) * HEAD] for source in range(sources)], axis=0
            ).astype(F32)
        )
        if kind < 3:
            qkv_out[:, kind * D : (kind + 1) * D] = lines
        else:
            pos_out[...] = lines
    for source in range(sources):
        for tile in range(4):
            at = 4 * HEAD + tile * share
            down_out[source * share : (source + 1) * share, tile * LANES : (tile + 1) * LANES] = all_ref[
                source, at : at + share
            ].astype(F32)


def late_kernel(*refs):
    part_refs = refs[:HEADS]
    (
        attn_gain_out,
        attn_bias_out,
        mlp_gain_out,
        mlp_bias_out,
        content_out,
        position_out,
        outw_out,
        up_out,
        up_bias_out,
        gain_out,
        bias_out,
        taps_out,
        conv_bias_out,
        down_bias_out,
        merge_out,
        merge_bias_out,
        all_s,
    ) = refs[HEADS:]
    place = lax.axis_index("tm")
    sources = all_s.shape[0]
    for apart, part_ref in enumerate(part_refs):
        all_s[lax.bitwise_xor(jnp.int32(apart), place)] = part_ref[...]
    channels = HALF // sources
    share = channels // 4

    def lines_at(base, size):
        return jnp.concatenate([all_s[source, base : base + size] for source in range(sources)], axis=0).astype(F32)

    for half in range(2):
        for group in range(4):
            at = half * HALF + group * sources * share
            up_out[:, at : at + sources * share] = jnp.transpose(
                lines_at(half * channels + group * share, share)
            )
    table = jnp.transpose(lines_at(2 * channels, share))
    taps_out[...] = table[:KERNEL]
    conv_bias_out[...] = table[KERNEL]
    gain_out[...] = table[KERNEL + 1]
    bias_out[...] = table[KERNEL + 2]
    wide = sources * share
    up_bias_out[:wide] = table[KERNEL + 3]
    up_bias_out[wide:] = table[KERNEL + 4]
    base = 2 * channels + share
    lines = all_s[0, base : base + 16].astype(F32)
    for source in range(1, sources):
        lines = lines + all_s[source, base : base + 16].astype(F32)
    outs = (attn_gain_out, attn_bias_out, mlp_gain_out, mlp_bias_out, content_out, position_out, down_bias_out, merge_bias_out)
    for line, out in enumerate(outs):
        out[...] = lines[line]
    base = base + 16
    merge_share = 2 * D // (4 * sources)
    head_share = D // (4 * sources)
    for source in range(sources):
        for tile in range(4):
            lanes = slice(tile * LANES, (tile + 1) * LANES)
            at = base + tile * merge_share
            merge_out[source * merge_share : (source + 1) * merge_share, lanes] = all_s[
                source, at : at + merge_share
            ].astype(F32)
            at = base + 4 * merge_share + tile * head_share
            outw_out[source * head_share : (source + 1) * head_share, lanes] = all_s[
                source, at : at + head_share
            ].astype(F32)


def moved(block, axis, bits):
    count = lax.axis_size(axis)
    return lax.ppermute(block, axis, [(index, index ^ bits) for index in range(count)])


def spread(block):
    near = [block] + [moved(block, "tm", bits) for bits in range(2, lax.axis_size("tm"), 2)]
    far = [moved(part, "tm", 1) for part in near]
    return [part for pair in zip(near, far) for part in pair]


def head_device(
    frames,
    lengths,
    cotangent,
    ln_attn_gain,
    ln_attn_bias,
    ln_mlp_gain,
    ln_mlp_bias,
    qkv_weight,
    content_bias,
    position_bias,
    pos_weight,
    out_weight,
    up_weight,
    up_bias,
    gate_norm_gain,
    gate_norm_bias,
    conv_kernel,
    conv_bias,
    down_weight,
    down_bias,
    merge_weight,
    merge_bias,
):
    count = lax.axis_size("tm")
    quarters = lax.axis_size("stream")
    own = frames.shape[1]
    total = own * count
    folded = total + total // 2
    padded = folded + 4 * MARGIN
    share = HALF // (quarters * count)
    channels = HALF // count
    quarter = D // quarters
    own_frames = frames[0]
    own_cotangent = cotangent[0]

    whole = Part()
    blocks = spread(own_frames)
    (gst_own,) = kernel_call(
        stats_kernel,
        [((own, D + LANES), BF16)],
        [*"vvvv", Part((D, HALF), lambda refs, buffer: [(refs[0].at[:, pl.ds(HALF, HALF)], buffer)]), "v"],
        [((own, HALF), F32)],
        micros=4,
    )(own_frames, own_cotangent, ln_mlp_gain, ln_mlp_bias, up_weight, up_bias)
    gst = [gst_own] + [moved(gst_own, "tm", bits) for bits in range(1, count)]
    up_own, table, qkv_own, pos_own, bias_own = kernel_call(
        select_kernel,
        [
            ((D, 3 * LANES), BF16),
            ((2, 8 + KERNEL + 1, LANES), F32),
            ((D, 3 * LANES), BF16),
            ((D, LANES), BF16),
            ((8, LANES), F32),
        ],
        10 * "v",
        micros=4,
    )(
        up_weight,
        up_bias,
        gate_norm_gain,
        gate_norm_bias,
        conv_bias,
        conv_kernel,
        qkv_weight,
        pos_weight,
        content_bias,
        position_bias,
    )
    frequency = jnp.exp(jnp.arange(D // 2, dtype=F32) * (-2.0 * math.log(10000.0) / D))
    coarse = jnp.arange(0, total, BLOCK, dtype=F32)[:, None] * frequency[None]
    fine = jnp.arange(BLOCK, dtype=F32)[:, None] * frequency[None]
    coarse_table = jnp.concatenate([jnp.sin(coarse), jnp.cos(coarse)], axis=1)
    fine_table = jnp.concatenate([jnp.sin(fine), jnp.cos(fine)], axis=1)

    n_attn, n_mlp, hat, q_position, query, key, value, prob, attn, row_share = kernel_call(
        attend_kernel,
        [
            ((total, D), BF16, 1),
            ((total, D), BF16, 1),
            ((total, D), BF16, 1),
            ((total, LANES), BF16, 1),
            ((total, LANES + D), BF16, 1),
            ((total, LANES + D), BF16, 1),
            ((total, LANES), BF16, 1),
            ((total, total), BF16, 1),
            ((total, LANES), F32, 1),
            ((total, LANES), F32, 1),
        ],
        ["s", blocks_part((0, D)), *"vvvvvvvvv"],
        bounds=True,
        micros=12,
    )(
        lengths,
        *blocks,
        ln_attn_gain,
        ln_attn_bias,
        ln_mlp_gain,
        ln_mlp_bias,
        qkv_own,
        pos_own,
        bias_own,
        coarse_table,
        fine_table,
    )

    def own_down(refs, buffer):
        place = lax.axis_index("tm")
        stride = HALF // quarters
        return [
            (
                refs[0].at[pl.ds(pl.multiple_of(part * stride + share * place, 16), share)],
                buffer.at[pl.ds(part * share, share)],
            )
            for part in range(quarters)
        ]

    mixed, gate_pre, grad_y, gate_hat, slope, down_pack, vectors, first_lines = kernel_call(
        mlp_first_kernel,
        [
            ((count, own + 16, 2 * LANES), BF16),
            ((folded, LANES), BF16, 1),
            ((folded, LANES), F32, 1),
            ((folded, LANES), F32, 1),
            ((folded, LANES), F32, 1),
            ((quarters, 4 * share, LANES), BF16),
            ((channels, LANES), F32),
            ((8, D), F32),
        ],
        [
            "s",
            whole,
            "v",
            "v",
            blocks_part((D, LANES)),
            blocks_part((0, D)),
            rows_part(D, D),
            Part((2 * LANES, D), own_down),
            whole,
        ],
        [
            ((folded, LANES), F32),
            ((folded, LANES), F32),
            ((padded, LANES), F32),
            ((padded, LANES), F32),
            ((folded, LANES), F32),
            ((folded, LANES), F32),
            ((total, D), BF16),
            ((total, 2 * LANES), BF16),
            ((2, 32, 8, LANES), F32),
            ((2, 32, 8, LANES), F32),
            ((2, 32, 8, LANES), F32),
            ((total, LANES), F32),
            ((3, WINDOW + 2 * MARGIN, LANES), F32),
            ((3, WINDOW + 2 * MARGIN, LANES), F32),
        ],
        bounds=True,
        micros=20,
    )(lengths, n_mlp, up_own, table, *gst, *gst, merge_weight, down_weight, attn)
    mixed_own = lax.all_to_all(mixed, "tm", 0, 0, tiled=True)

    def own_head(refs, buffer):
        at = pl.ds(pl.multiple_of(lax.axis_index("tm") * HEAD, HEAD), HEAD)
        return [(refs[0].at[at], buffer.at[pl.ds(0, HEAD)])]

    branch, from_attn, *head_packs, head_lines = kernel_call(
        attend_back_kernel,
        [((total, D), BF16, 1), ((total, D), BF16, 1)]
        + [((512, LANES), BF16)] * quarters
        + [((8, D), F32)],
        [
            blocks_part((0, D)),
            rows_part(0, D),
            Part((LANES, D), own_head),
            whole,
            whole,
            whole,
            whole,
            whole,
            "v",
            "v",
            whole,
            Part((total, LANES), lambda refs, buffer: [(refs[0].at[:, pl.ds(0, LANES)], buffer)]),
            whole,
            whole,
            whole,
            whole,
            "v",
            "v",
        ],
        [
            ((total, LANES), BF16),
            ((total, total), BF16),
            ((total, D), BF16),
            ((total, 3 * LANES), BF16),
            ((4 * HEAD, D), F32),
        ],
        micros=14,
    )(
        *gst,
        merge_weight,
        out_weight,
        row_share,
        value,
        attn,
        prob,
        key,
        coarse_table,
        fine_table,
        pos_own,
        query,
        n_attn,
        q_position,
        qkv_own,
        hat,
        ln_attn_gain,
        down_pack,
    )
    head_parts = [head_packs[0]] + [moved(head_packs[bits], "stream", bits) for bits in range(1, quarters)]
    (head_part,) = kernel_call(add_kernel, [((512, LANES), BF16)], quarters * "v", micros=1)(*head_parts)
    head_all = lax.all_gather(head_part, "tm", axis=0)

    out_rows, joined = kernel_call(
        output_kernel,
        [((own, D), BF16), ((count, 256, own), BF16)],
        "vvvvvvv",
    )(own_frames, mixed_own, out_weight, down_weight, down_bias, merge_weight, merge_bias)
    joined_all = lax.all_to_all(joined, "tm", 0, 0, tiled=True)

    pack_rows = 9 * share + 16
    same, apart, *up_packs = kernel_call(
        mlp_second_kernel,
        [((count // 2, own, D), BF16)] * 2 + [((pack_rows, LANES), BF16)] * quarters,
        ["v", blocks_part((D, LANES)), *([whole] * 6), "v", whole, whole, *"vvv"],
        [
            ((total, 3 * LANES), BF16),
            ((total, LANES), F32),
            ((3 * LANES, D), F32),
            ((16, D), F32),
            ((channels, LANES), F32),
        ],
        micros=10,
    )(
        mixed_own,
        *gst,
        gate_pre,
        grad_y,
        gate_hat,
        slope,
        up_own,
        hat,
        ln_mlp_gain,
        from_attn,
        n_mlp,
        vectors,
        first_lines,
        head_lines,
    )
    sibling = moved(apart, "tm", 1)
    up_parts = [up_packs[0]] + [moved(up_packs[bits], "stream", bits) for bits in range(1, quarters)]
    merge_rows = 3 * D // count
    merge_packs = kernel_call(
        merge_kernel,
        [((merge_rows, LANES), BF16)] * quarters,
        ["v", blocks_part((0, D)), whole],
        [((2 * D // count, D), F32), ((D // count, D), F32)],
        micros=3,
    )(joined_all, *gst, branch)
    merge_parts = [merge_packs[0]] + [moved(merge_packs[bits], "stream", bits) for bits in range(1, quarters)]
    pairs = kernel_call(pair_kernel, [((own, D), BF16)] * (count // 2), "vv", micros=1)(same, sibling)
    sums = [pairs[0]] + [moved(pairs[slot], "tm", 2 * slot) for slot in range(1, count // 2)]
    (late_part,) = kernel_call(
        add_kernel, [((pack_rows + merge_rows, LANES), BF16)], 2 * quarters * "v", micros=1
    )(*up_parts, *merge_parts)
    late_parts = spread(late_part)
    (grad_frames,) = kernel_call(frames_kernel, [((own, D), F32)], (2 + count // 2) * "v")(
        own_frames, own_cotangent, *sums
    )
    grad_qkv, grad_pos, grad_down = kernel_call(
        early_kernel,
        [((quarter, 3 * D), F32), ((quarter, D), F32), ((HALF // quarters, D), F32)],
        "v",
    )(head_all)
    late = kernel_call(
        late_kernel,
        [((quarter,), F32)] * 6
        + [
            ((quarter, D), F32),
            ((quarter, 2 * HALF), F32),
            ((2 * HALF // quarters,), F32),
            ((HALF // quarters,), F32),
            ((HALF // quarters,), F32),
            ((KERNEL, HALF // quarters), F32),
            ((HALF // quarters,), F32),
            ((quarter,), F32),
            ((2 * D // quarters, D), F32),
            ((quarter,), F32),
        ],
        count * "v",
        [((count,) + late_part.shape, BF16)],
        micros=3,
    )(*late_parts)
    return (
        (out_rows[None], grad_frames[None])
        + tuple(late[:4])
        + (grad_qkv,)
        + tuple(late[4:6])
        + (grad_pos,)
        + tuple(late[6:13])
        + (grad_down,)
        + tuple(late[13:])
    )


def per_device(*operands):
    fits = (
        lax.axis_size("tm") == HEADS
        and lax.axis_size("stream") * LANES == D
        and operands[0].shape[1] == BLOCK
    )
    return head_device(*operands) if fits else frame_device(*operands)


def solution(mesh):
    return jax.shard_map(
        per_device,
        mesh=mesh,
        in_specs=(
            P("stream", "tm", None),
            P("stream", None),
            P("stream", "tm", None),
            P(),
            P(),
            P(),
            P(),
            P(),
            P(),
            P(),
            P(),
            P(),
            P(),
            P(),
            P(),
            P(),
            P(),
            P(),
            P(),
            P(),
            P(),
            P(),
        ),
        out_specs=(
            P("stream", "tm", None),
            P("stream", "tm", None),
            P("stream"),
            P("stream"),
            P("stream"),
            P("stream"),
            P("stream", None),
            P("stream"),
            P("stream"),
            P("stream", None),
            P("stream", None),
            P("stream", None),
            P("stream"),
            P("stream"),
            P("stream"),
            P(None, "stream"),
            P("stream"),
            P("stream", None),
            P("stream"),
            P("stream", None),
            P("stream"),
        ),
        check_vma=False,
    )
```

```python
import math

import jax
import jax.numpy as jnp
from jax import lax
from jax.experimental import pallas as pl
from jax.experimental.pallas import tpu as pltpu
from jax.sharding import PartitionSpec as P

D = 512
HEADS = 8
HEAD = 64
KERNEL = 31
ITEMS = 5
HALF = 1536


EPS = 1e-05
MASKED = -1e30


def extended(block, sides, width):
    for axis, dim in sides:
        count = lax.axis_size(axis)
        forward = [(i, i + 1) for i in range(count - 1)]
        backward = [(target, source) for source, target in forward]
        low = lax.ppermute(
            lax.slice_in_dim(block, block.shape[dim] - width, None, axis=dim), axis, forward
        )
        high = lax.ppermute(lax.slice_in_dim(block, 0, width, axis=dim), axis, backward)
        block = jnp.concatenate([low, block, high], axis=dim)
    return block


def norm_rows(inputs, scale_row, shift_row):
    row_mean = jnp.mean(inputs, axis=-1, keepdims=True)
    centred = inputs - row_mean
    spread = jnp.mean(centred * centred, axis=-1, keepdims=True)
    return centred * lax.rsqrt(spread + EPS) * scale_row + shift_row


def gelu_exact(inputs):
    return jax.nn.gelu(inputs, approximate=False)


def frame_info(lengths, offset, extent):
    item_ends = jnp.cumsum(lengths)
    first_table = jnp.concatenate([item_ends - lengths, item_ends[-1:]])
    frame_index = offset + jnp.arange(extent, dtype=jnp.int32)
    item_of = jnp.sum((frame_index[:, None] >= item_ends[None, :]).astype(jnp.int32), axis=1)
    labels = jnp.arange(ITEMS + 1, dtype=jnp.int32)
    first_frame = jnp.sum(
        jnp.where(item_of[:, None] == labels[None, :], first_table[None, :], 0), axis=1
    )
    return (frame_index, item_of, frame_index - first_frame)


def angles(place_in):
    frequency = jnp.exp(jnp.arange(D // 2, dtype=jnp.float32) * (-2.0 * math.log(10000.0) / D))
    phase_angle = place_in.astype(jnp.float32)[:, None] * frequency[None, :]
    return (jnp.sin(phase_angle), jnp.cos(phase_angle))


def rel_query(projected, sine_rows, cosine_rows):
    half_size = projected.shape[-1] // 2
    first_half = projected[..., :half_size]
    second_half = projected[..., half_size:]
    sine_wide = sine_rows[:, None, :]
    cosine_wide = cosine_rows[:, None, :]
    return jnp.concatenate(
        [
            first_half * sine_wide + second_half * cosine_wide,
            second_half * sine_wide - first_half * cosine_wide,
        ],
        axis=-1,
    )


def step_size(extent):
    return math.gcd(extent, 512)


def score_block(q_content, q_rel, query_item, query_frame, key_block, key_start, lengths):
    extent = key_block.shape[0]
    key_frame, key_item, key_place = frame_info(lengths, key_start, extent)
    sine_rows, cosine_rows = angles(key_place)
    k_rel = jnp.concatenate([cosine_rows, sine_rows], axis=1).astype(jnp.bfloat16)
    raw_scores = jnp.einsum(
        "qhe,khe->hqk",
        q_content,
        key_block.reshape(extent, HEADS, HEAD),
        preferred_element_type=jnp.float32,
    )
    raw_scores = raw_scores + jnp.einsum(
        "qhc,kc->hqk", q_rel, k_rel, preferred_element_type=jnp.float32
    )
    allowed = (query_item[:, None] == key_item[None, :]) & (
        (query_item[:, None] < ITEMS) | (query_frame[:, None] == key_frame[None, :])
    )
    return (raw_scores, allowed, k_rel)


def block_grads(
    q_content,
    q_rel,
    query_item,
    query_frame,
    grad_out,
    log_total,
    delta_rows,
    key_block,
    value_block,
    key_start,
    lengths,
):
    extent = key_block.shape[0]
    raw_scores, allowed, k_rel = score_block(
        q_content, q_rel, query_item, query_frame, key_block, key_start, lengths
    )
    prob_rows = jnp.where(allowed[None], jnp.exp(raw_scores * 0.125 - log_total[:, :, None]), 0.0)
    grad_prob = jnp.einsum(
        "qhe,khe->hqk",
        grad_out,
        value_block.reshape(extent, HEADS, HEAD),
        preferred_element_type=jnp.float32,
    )
    grad_raw = (prob_rows * (grad_prob - delta_rows[:, :, None]) * 0.125).astype(jnp.bfloat16)
    return (prob_rows.astype(jnp.bfloat16), grad_raw, k_rel)


def frame_device(
    frames,
    lengths,
    cotangent,
    ln_attn_gain,
    ln_attn_bias,
    ln_mlp_gain,
    ln_mlp_bias,
    qkv_weight,
    content_bias,
    position_bias,
    pos_weight,
    out_weight,
    up_weight,
    up_bias,
    gate_norm_gain,
    gate_norm_bias,
    conv_kernel,
    conv_bias,
    down_weight,
    down_bias,
    merge_weight,
    merge_bias,
):
    row_count = frames.shape[1]
    cycle_size = lax.axis_size("tm")
    offset = lax.axis_index("tm") * row_count
    stream_lengths = lengths[0]
    inputs = frames[0].astype(jnp.float32)
    frame_index, item_of, place_in = frame_info(stream_lengths, offset, row_count)
    sine_rows, cosine_rows = angles(place_in)
    attn_norm, attn_pull = jax.vjp(
        norm_rows, inputs, ln_attn_gain.astype(jnp.float32), ln_attn_bias.astype(jnp.float32)
    )
    mlp_norm, mlp_pull = jax.vjp(
        norm_rows, inputs, ln_mlp_gain.astype(jnp.float32), ln_mlp_bias.astype(jnp.float32)
    )
    attn_norm_low = attn_norm.astype(jnp.bfloat16)
    mlp_norm_low = mlp_norm.astype(jnp.bfloat16)
    qkv_rows = jnp.dot(attn_norm_low, qkv_weight, preferred_element_type=jnp.float32)
    query_rows = qkv_rows[:, :D]
    key_rows = qkv_rows[:, D : 2 * D].astype(jnp.bfloat16)
    value_rows = qkv_rows[:, 2 * D :].astype(jnp.bfloat16)
    q_content = (query_rows + content_bias.astype(jnp.float32)).astype(jnp.bfloat16)
    q_position = (query_rows + position_bias.astype(jnp.float32)).astype(jnp.bfloat16)
    content_heads = q_content.reshape(row_count, HEADS, HEAD)
    position_heads = q_position.reshape(row_count, HEADS, HEAD)
    pos_heads = pos_weight.reshape(D, HEADS, HEAD)
    projected = jnp.einsum(
        "the,che->thc", position_heads, pos_heads, preferred_element_type=jnp.float32
    )
    q_rel = rel_query(projected, sine_rows, cosine_rows).astype(jnp.bfloat16)
    start_state = (
        jnp.full((HEADS, row_count), MASKED, jnp.float32),
        jnp.zeros((HEADS, row_count), jnp.float32),
        jnp.zeros((HEADS, row_count, HEAD), jnp.float32),
    )
    fold_state = start_state
    key_piece = lax.all_gather(key_rows, "tm", axis=0, tiled=True)
    value_piece = lax.all_gather(value_rows, "tm", axis=0, tiled=True)
    extent = key_piece.shape[0]
    step_rows = step_size(extent)

    def forward_one_step(inner_state, step_index):
        row_top, row_total, row_acc = inner_state
        key_block = lax.dynamic_slice_in_dim(key_piece, step_index * step_rows, step_rows, 0)
        value_block = lax.dynamic_slice_in_dim(value_piece, step_index * step_rows, step_rows, 0)
        raw_scores, allowed, k_rel = score_block(
            content_heads,
            q_rel,
            item_of,
            frame_index,
            key_block,
            step_index * step_rows,
            stream_lengths,
        )
        scaled = jnp.where(allowed[None], raw_scores * 0.125, MASKED)
        new_top = jnp.maximum(row_top, jnp.max(scaled, axis=2))
        weight = jnp.where(allowed[None], jnp.exp(scaled - new_top[:, :, None]), 0.0)
        factor = jnp.exp(row_top - new_top)
        row_total = row_total * factor + jnp.sum(weight, axis=2)
        row_acc = row_acc * factor[:, :, None] + jnp.einsum(
            "hqk,khe->hqe",
            weight.astype(jnp.bfloat16),
            value_block.reshape(step_rows, HEADS, HEAD),
            preferred_element_type=jnp.float32,
        )
        return ((new_top, row_total, row_acc), None)

    fold_state, unused = lax.scan(
        forward_one_step, fold_state, jnp.arange(extent // step_rows, dtype=jnp.int32)
    )
    row_top, row_total, row_acc = fold_state
    attn_heads = row_acc / row_total[:, :, None]
    log_total = row_top + jnp.log(row_total)
    attn_low = jnp.transpose(attn_heads, (1, 0, 2)).reshape(row_count, D).astype(jnp.bfloat16)
    branch_attn = jnp.dot(attn_low, out_weight, preferred_element_type=jnp.float32).astype(
        jnp.bfloat16
    )
    hidden_pre = jnp.dot(
        mlp_norm_low, up_weight, preferred_element_type=jnp.float32
    ) + up_bias.astype(jnp.float32)
    hidden, gelu_pull = jax.vjp(gelu_exact, hidden_pre)
    gate_half = hidden[:, :HALF]
    conv_norm, conv_pull = jax.vjp(
        norm_rows,
        hidden[:, HALF:],
        gate_norm_gain.astype(jnp.float32),
        gate_norm_bias.astype(jnp.float32),
    )
    conv_in = conv_norm.astype(jnp.bfloat16)
    half_width = KERNEL // 2
    conv_wide = extended(conv_in, (("tm", 0),), half_width)
    wide_frame, wide_item, wide_place = frame_info(
        stream_lengths, offset - half_width, row_count + 2 * half_width
    )
    kernel_rows = conv_kernel.astype(jnp.float32)
    conv_out = conv_bias.astype(jnp.float32) + jnp.zeros_like(gate_half)
    for tap_index in range(KERNEL):
        same_item = (wide_item[tap_index : tap_index + row_count] == item_of)[:, None]
        conv_out = (
            conv_out
            + jnp.where(
                same_item, conv_wide[tap_index : tap_index + row_count].astype(jnp.float32), 0.0
            )
            * kernel_rows[tap_index]
        )
    gated_low = (gate_half * conv_out).astype(jnp.bfloat16)
    branch_mlp = (
        jnp.dot(gated_low, down_weight, preferred_element_type=jnp.float32)
        + down_bias.astype(jnp.float32)
    ).astype(jnp.bfloat16)
    joined = jnp.concatenate([branch_attn, branch_mlp], axis=1)
    result = (
        inputs
        + jnp.dot(joined, merge_weight, preferred_element_type=jnp.float32)
        + merge_bias.astype(jnp.float32)
    )
    out_rows = result.astype(jnp.bfloat16)[None]
    grad_low = cotangent[0]
    grad_rows = grad_low.astype(jnp.float32)
    grad_merge_bias = jnp.sum(grad_rows, axis=0)
    grad_merge_weight = jnp.einsum(
        "tc,td->cd", joined, grad_low, preferred_element_type=jnp.float32
    )
    grad_joined = jnp.einsum(
        "td,cd->tc", grad_low, merge_weight, preferred_element_type=jnp.float32
    )
    grad_attn_branch = grad_joined[:, :D].astype(jnp.bfloat16)
    grad_mlp_branch = grad_joined[:, D:].astype(jnp.bfloat16)
    grad_down_weight = jnp.einsum(
        "tc,td->cd", gated_low, grad_mlp_branch, preferred_element_type=jnp.float32
    )
    grad_down_bias = jnp.sum(grad_mlp_branch.astype(jnp.float32), axis=0)
    grad_gated = jnp.einsum(
        "td,cd->tc", grad_mlp_branch, down_weight, preferred_element_type=jnp.float32
    )
    grad_gate_half = grad_gated * conv_out
    grad_conv_out = (grad_gated * gate_half).astype(jnp.bfloat16)
    grad_conv_rows = grad_conv_out.astype(jnp.float32)
    grad_conv_bias = jnp.sum(grad_conv_rows, axis=0)
    grad_wide = extended(grad_conv_out, (("tm", 0),), half_width)
    kernel_list = []
    grad_conv_in = jnp.zeros_like(grad_conv_rows)
    for tap_index in range(KERNEL):
        same_item = (wide_item[tap_index : tap_index + row_count] == item_of)[:, None]
        kernel_list.append(
            jnp.sum(
                jnp.where(
                    same_item, conv_wide[tap_index : tap_index + row_count].astype(jnp.float32), 0.0
                )
                * grad_conv_rows,
                axis=0,
            )
        )
        back_start = 2 * half_width - tap_index
        back_item = (wide_item[back_start : back_start + row_count] == item_of)[:, None]
        grad_conv_in = (
            grad_conv_in
            + jnp.where(
                back_item, grad_wide[back_start : back_start + row_count].astype(jnp.float32), 0.0
            )
            * kernel_rows[tap_index]
        )
    grad_conv_kernel = jnp.stack(kernel_list)
    grad_second, grad_gate_norm_gain, grad_gate_norm_bias = conv_pull(grad_conv_in)
    (grad_pre_rows,) = gelu_pull(jnp.concatenate([grad_gate_half, grad_second], axis=1))
    grad_pre = grad_pre_rows.astype(jnp.bfloat16)
    grad_up_bias = jnp.sum(grad_pre.astype(jnp.float32), axis=0)
    grad_up_weight = jnp.einsum(
        "tc,tf->cf", mlp_norm_low, grad_pre, preferred_element_type=jnp.float32
    )
    grad_mlp_norm = jnp.einsum("tf,cf->tc", grad_pre, up_weight, preferred_element_type=jnp.float32)
    grad_out_weight = jnp.einsum(
        "tc,td->cd", attn_low, grad_attn_branch, preferred_element_type=jnp.float32
    )
    grad_attn_low = jnp.einsum(
        "td,cd->tc", grad_attn_branch, out_weight, preferred_element_type=jnp.float32
    ).astype(jnp.bfloat16)
    grad_out_heads = grad_attn_low.reshape(row_count, HEADS, HEAD)
    delta_rows = jnp.sum(
        jnp.transpose(grad_out_heads.astype(jnp.float32), (1, 0, 2)) * attn_heads, axis=2
    )
    total_frames = row_count * cycle_size
    back_start_state = (
        jnp.zeros((row_count, HEADS, HEAD), jnp.float32),
        jnp.zeros((row_count, HEADS, D), jnp.float32),
        jnp.zeros((total_frames, D), jnp.float32),
        jnp.zeros((total_frames, D), jnp.float32),
    )
    back_key_piece = lax.all_gather(key_rows, "tm", axis=0, tiled=True)
    back_value_piece = lax.all_gather(value_rows, "tm", axis=0, tiled=True)
    extent = back_key_piece.shape[0]
    back_step_rows = step_size(extent)

    def back_one_step(inner_state, step_index):
        grad_content, grad_rel = inner_state
        key_block = lax.dynamic_slice_in_dim(
            back_key_piece, step_index * back_step_rows, back_step_rows, 0
        )
        value_block = lax.dynamic_slice_in_dim(
            back_value_piece, step_index * back_step_rows, back_step_rows, 0
        )
        prob_low, grad_raw, k_rel = block_grads(
            content_heads,
            q_rel,
            item_of,
            frame_index,
            grad_out_heads,
            log_total,
            delta_rows,
            key_block,
            value_block,
            step_index * back_step_rows,
            stream_lengths,
        )
        grad_content = grad_content + jnp.einsum(
            "hqk,khe->qhe",
            grad_raw,
            key_block.reshape(back_step_rows, HEADS, HEAD),
            preferred_element_type=jnp.float32,
        )
        grad_rel = grad_rel + jnp.einsum(
            "hqk,kc->qhc", grad_raw, k_rel, preferred_element_type=jnp.float32
        )
        key_part = jnp.einsum(
            "hqk,qhe->khe", grad_raw, content_heads, preferred_element_type=jnp.float32
        ).reshape(back_step_rows, D)
        value_part = jnp.einsum(
            "hqk,qhe->khe", prob_low, grad_out_heads, preferred_element_type=jnp.float32
        ).reshape(back_step_rows, D)
        return ((grad_content, grad_rel), (key_part, value_part))

    inner_state, block_parts = lax.scan(
        back_one_step,
        (back_start_state[0], back_start_state[1]),
        jnp.arange(extent // back_step_rows, dtype=jnp.int32),
    )
    key_all = block_parts[0].reshape(extent, D)
    value_all = block_parts[1].reshape(extent, D)
    grad_content, grad_rel, key_all, value_all = (
        inner_state[0],
        inner_state[1],
        key_all,
        value_all,
    )
    grad_keys, grad_values = (
        lax.psum_scatter(key_all, "tm", scatter_dimension=0, tiled=True),
        lax.psum_scatter(value_all, "tm", scatter_dimension=0, tiled=True),
    )
    half_size = D // 2
    rel_first = grad_rel[..., :half_size]
    rel_second = grad_rel[..., half_size:]
    sine_wide = sine_rows[:, None, :]
    cosine_wide = cosine_rows[:, None, :]
    grad_projected = jnp.concatenate(
        [
            rel_first * sine_wide - rel_second * cosine_wide,
            rel_first * cosine_wide + rel_second * sine_wide,
        ],
        axis=-1,
    ).astype(jnp.bfloat16)
    grad_pos_weight = jnp.einsum(
        "thc,the->che", grad_projected, position_heads, preferred_element_type=jnp.float32
    ).reshape(D, D)
    grad_q_position = jnp.einsum(
        "thc,che->the", grad_projected, pos_heads, preferred_element_type=jnp.float32
    )
    grad_content_bias = jnp.sum(grad_content, axis=0).reshape(D)
    grad_position_bias = jnp.sum(grad_q_position, axis=0).reshape(D)
    grad_query = (grad_content + grad_q_position).reshape(row_count, D).astype(jnp.bfloat16)
    grad_qkv = jnp.concatenate(
        [grad_query, grad_keys.astype(jnp.bfloat16), grad_values.astype(jnp.bfloat16)], axis=1
    )
    grad_qkv_weight = jnp.einsum(
        "tc,tf->cf", attn_norm_low, grad_qkv, preferred_element_type=jnp.float32
    )
    grad_attn_norm = jnp.einsum(
        "tf,cf->tc", grad_qkv, qkv_weight, preferred_element_type=jnp.float32
    )
    grad_from_attn, grad_ln_attn_gain, grad_ln_attn_bias = attn_pull(grad_attn_norm)
    grad_from_mlp, grad_ln_mlp_gain, grad_ln_mlp_bias = mlp_pull(grad_mlp_norm)
    grad_inputs = grad_rows + grad_from_attn + grad_from_mlp
    weight_grads = (
        grad_ln_attn_gain,
        grad_ln_attn_bias,
        grad_ln_mlp_gain,
        grad_ln_mlp_bias,
        grad_qkv_weight,
        grad_content_bias,
        grad_position_bias,
        grad_pos_weight,
        grad_out_weight,
        grad_up_weight,
        grad_up_bias,
        grad_gate_norm_gain,
        grad_gate_norm_bias,
        grad_conv_kernel,
        grad_conv_bias,
        grad_down_weight,
        grad_down_bias,
        grad_merge_weight,
        grad_merge_bias,
    )
    summed = lax.psum(
        (
            weight_grads[0],
            weight_grads[1],
            weight_grads[2],
            weight_grads[3],
            weight_grads[4],
            weight_grads[5],
            weight_grads[6],
            weight_grads[7],
            weight_grads[8],
            weight_grads[9],
            weight_grads[10],
            weight_grads[11],
            weight_grads[12],
            weight_grads[13],
            weight_grads[14],
            weight_grads[15],
            weight_grads[16],
            weight_grads[17],
            weight_grads[18],
        ),
        "tm",
    )
    shares = (
        lax.psum_scatter(
            summed[0].astype(jnp.bfloat16), "stream", scatter_dimension=0, tiled=True
        ).astype(jnp.float32),
        lax.psum_scatter(
            summed[1].astype(jnp.bfloat16), "stream", scatter_dimension=0, tiled=True
        ).astype(jnp.float32),
        lax.psum_scatter(
            summed[2].astype(jnp.bfloat16), "stream", scatter_dimension=0, tiled=True
        ).astype(jnp.float32),
        lax.psum_scatter(
            summed[3].astype(jnp.bfloat16), "stream", scatter_dimension=0, tiled=True
        ).astype(jnp.float32),
        lax.psum_scatter(
            summed[4].astype(jnp.bfloat16), "stream", scatter_dimension=0, tiled=True
        ).astype(jnp.float32),
        lax.psum_scatter(
            summed[5].astype(jnp.bfloat16), "stream", scatter_dimension=0, tiled=True
        ).astype(jnp.float32),
        lax.psum_scatter(
            summed[6].astype(jnp.bfloat16), "stream", scatter_dimension=0, tiled=True
        ).astype(jnp.float32),
        lax.psum_scatter(
            summed[7].astype(jnp.bfloat16), "stream", scatter_dimension=0, tiled=True
        ).astype(jnp.float32),
        lax.psum_scatter(
            summed[8].astype(jnp.bfloat16), "stream", scatter_dimension=0, tiled=True
        ).astype(jnp.float32),
        lax.psum_scatter(
            summed[9].astype(jnp.bfloat16), "stream", scatter_dimension=0, tiled=True
        ).astype(jnp.float32),
        lax.psum_scatter(
            summed[10].astype(jnp.bfloat16), "stream", scatter_dimension=0, tiled=True
        ).astype(jnp.float32),
        lax.psum_scatter(
            summed[11].astype(jnp.bfloat16), "stream", scatter_dimension=0, tiled=True
        ).astype(jnp.float32),
        lax.psum_scatter(
            summed[12].astype(jnp.bfloat16), "stream", scatter_dimension=0, tiled=True
        ).astype(jnp.float32),
        lax.psum_scatter(
            summed[13].astype(jnp.bfloat16), "stream", scatter_dimension=1, tiled=True
        ).astype(jnp.float32),
        lax.psum_scatter(
            summed[14].astype(jnp.bfloat16), "stream", scatter_dimension=0, tiled=True
        ).astype(jnp.float32),
        lax.psum_scatter(
            summed[15].astype(jnp.bfloat16), "stream", scatter_dimension=0, tiled=True
        ).astype(jnp.float32),
        lax.psum_scatter(
            summed[16].astype(jnp.bfloat16), "stream", scatter_dimension=0, tiled=True
        ).astype(jnp.float32),
        lax.psum_scatter(
            summed[17].astype(jnp.bfloat16), "stream", scatter_dimension=0, tiled=True
        ).astype(jnp.float32),
        lax.psum_scatter(
            summed[18].astype(jnp.bfloat16), "stream", scatter_dimension=0, tiled=True
        ).astype(jnp.float32),
    )
    return (out_rows, grad_inputs[None]) + tuple(shares)


LANES = 128
LOW = LANES // 2
BLOCK = 128
TALL = 256
WINDOW = 64
MARGIN = 16
BOUNDS = 16
MEGA = 1024 * 1024
RATE = 1150000000
F32 = jnp.float32
BF16 = jnp.bfloat16


def dot_nn(left, right):
    return jnp.dot(left, right, preferred_element_type=F32)


def dot_nt(left, right):
    return lax.dot_general(left, right, (((1,), (1,)), ((), ())), preferred_element_type=F32)


def dot_tn(left, right):
    return lax.dot_general(left, right, (((0,), (0,)), ((), ())), preferred_element_type=F32)


def rows_of(index, size, base=0):
    return pl.ds(pl.multiple_of(index * size, size) + base, size)


def line_of(ref):
    return ref[...].astype(F32).reshape(1, ref.shape[0])


def fold_rows(values):
    return jnp.sum(values.reshape(values.shape[0] // 8, 8, values.shape[1]), axis=0)


def one_row(values):
    return jnp.sum(values, axis=0, keepdims=True)


def turn(values):
    return pltpu.roll(values, LOW, 1)


def low_lanes(rows):
    return lax.broadcasted_iota(jnp.int32, (rows, LANES), 1) < LOW


def centre_rows(inputs):
    mean = jnp.mean(inputs, axis=-1, keepdims=True)
    centred = inputs - mean
    spread = jnp.mean(centred * centred, axis=-1, keepdims=True)
    return centred * lax.rsqrt(spread + EPS)


ERF_SCALE = 0.3275911 / math.sqrt(2.0)
ERF_TERMS = tuple(0.5 * term for term in (1.061405429, -1.453152027, 1.421413741, -0.284496736, 0.254829592))


def normal_parts(values):
    bell = jnp.exp(values * values * -0.5)
    size = 1.0 + ERF_SCALE * jnp.abs(values)
    place = pl.reciprocal(size, approx=True)
    place = place * (2.0 - size * place)
    series = ERF_TERMS[0]
    for term in ERF_TERMS[1:]:
        series = series * place + term
    tail = series * place * bell
    return jnp.where(values < 0.0, tail, 1.0 - tail), bell


def gelu_parts(values):
    phi, bell = normal_parts(values)
    return values * phi, phi + values * bell * (1.0 / math.sqrt(2.0 * math.pi))


class Part:
    def __init__(self, shape=None, pairs=None, refs=1):
        self.shape, self.pairs, self.refs = shape, pairs, refs

    def buffer(self, operand):
        return self.shape or operand.shape

    def copies(self, refs, buffer):
        return self.pairs(refs, buffer) if self.pairs else [(refs[0], buffer)]


def blocks_part():
    def pairs(refs, buffer):
        place = lax.axis_index("tm")
        return [
            (ref, buffer.at[rows_of(lax.bitwise_xor(jnp.int32(apart), place), BLOCK)])
            for apart, ref in enumerate(refs)
        ]

    return Part((HEADS * BLOCK, D), pairs, HEADS)


def rows_part(first, size):
    return Part((size, D), lambda refs, buffer: [(refs[0].at[pl.ds(first, size)], buffer)])


class Fetch:
    def __init__(self, pairs, buffer, sems, first):
        self.buffer = buffer
        self.pending = [
            pltpu.make_async_copy(source, target, sems.at[first + index])
            for index, (source, target) in enumerate(pairs)
        ]
        for copy in self.pending:
            copy.start()

    def __call__(self):
        for copy in self.pending:
            copy.wait()
        self.pending = []
        return self.buffer


class Send:
    def __init__(self, buffer, target, sem):
        self.buffer, self.copy, self.begun = buffer, pltpu.make_async_copy(buffer, target, sem), False

    def go(self):
        if not self.begun:
            self.copy.start()
        self.begun = True


SPACES = {"v": pltpu.VMEM, "s": pltpu.SMEM, "k": pl.ANY}


def kernel_call(body, out_shapes, plan, scratch=(), micros=2, megas=58, bounds=False, aliases=None):
    def call(*operands):
        in_specs, buffers, at = [], [], 0
        for item in plan:
            if isinstance(item, Part):
                in_specs += [pl.BlockSpec(memory_space=pl.ANY)] * item.refs
                buffers.append(pltpu.VMEM(item.buffer(operands[at]), operands[at].dtype))
                at += item.refs
            else:
                in_specs.append(pl.BlockSpec(memory_space=SPACES[item]))
                at += 1
        sent = [out for out in out_shapes if len(out) > 2]
        buffers += [pltpu.VMEM(out[3] if len(out) > 3 else out[0], out[1]) for out in sent]
        sem_count = 64
        extra = [pltpu.SMEM((BOUNDS,), jnp.int32)] if bounds else []

        def outer(*refs):
            inputs, rest = refs[: len(in_specs)], refs[len(in_specs) :]
            outputs, rest = rest[: len(out_shapes)], rest[len(out_shapes) :]
            held, rest = list(rest[: len(buffers)]), rest[len(buffers) :]
            sems, rest = rest[0], rest[1:]
            given, at, used = [], 0, 0
            for item in plan:
                if isinstance(item, Part):
                    buffer = held.pop(0)
                    pairs = item.copies(inputs[at : at + item.refs], buffer)
                    given.append(Fetch(pairs, buffer, sems, used))
                    used += len(pairs)
                    at += item.refs
                else:
                    given.append(inputs[at])
                    at += 1
            results = []
            for out, ref in zip(out_shapes, outputs):
                if len(out) > 2:
                    target = out[4](ref) if len(out) > 3 else ref
                    results.append(Send(held.pop(0), target, sems.at[used]))
                    used += 1
                else:
                    results.append(ref)
            assert used <= sem_count
            body(*given, *results, *rest)
            for item in given:
                if isinstance(item, Fetch):
                    item()
            sends = [item for item in results if isinstance(item, Send)]
            for item in sends:
                item.go()
            for item in sends:
                item.copy.wait()

        return pl.pallas_call(
            outer,
            out_shape=[jax.ShapeDtypeStruct(out[0], out[1]) for out in out_shapes],
            in_specs=in_specs,
            out_specs=[pl.BlockSpec(memory_space=pl.ANY if len(out) > 2 else pltpu.VMEM) for out in out_shapes],
            scratch_shapes=buffers
            + [pltpu.SemaphoreType.DMA((sem_count,))]
            + [pltpu.VMEM(shape, kind) for shape, kind in scratch]
            + extra,
            input_output_aliases=aliases or {},
            compiler_params=pltpu.CompilerParams(vmem_limit_bytes=megas * MEGA),
            cost_estimate=pl.CostEstimate(flops=micros * RATE, bytes_accessed=1 << 20, transcendentals=0),
        )(*operands)

    return call


def fill_bounds(lengths_ref, bounds_s, total):
    bounds_s[0] = jnp.int32(0)
    end = jnp.int32(0)
    for item in range(ITEMS):
        end = end + lengths_ref[0, item]
        bounds_s[item + 1] = end
    for item in range(ITEMS + 1, BOUNDS):
        bounds_s[item] = jnp.int32(total)


def select_kernel(
    up_ref,
    up_bias_ref,
    gain_ref,
    bias_ref,
    conv_bias_ref,
    taps_ref,
    qkv_ref,
    pos_ref,
    content_ref,
    position_ref,
    up_out,
    table_out,
    qkv_out,
    pos_out,
    bias_out,
):
    place = lax.axis_index("tm")
    quarters = lax.axis_size("stream")
    share = HALF // (quarters * lax.axis_size("tm"))
    lane = lax.broadcasted_iota(jnp.int32, (1, 2 * LANES), 1)
    channel = jnp.where(lane < LANES + LOW, lane, lane - LOW)
    group = jnp.zeros_like(channel)
    for quarter in range(1, quarters):
        group = group + (channel >= quarter * share).astype(jnp.int32)
    source = group * (HALF // quarters) + share * place + channel - group * share
    chosen = (lax.broadcasted_iota(jnp.int32, (HALF, 2 * LANES), 0) == source).astype(F32).astype(BF16)
    gate = dot_nn(up_ref[:, :HALF], chosen)
    conv = dot_nn(up_ref[:, HALF:], chosen)
    up_out[:, :LANES] = gate[:, :LANES].astype(BF16)
    up_out[:, LANES : 2 * LANES] = jnp.where(low_lanes(D), gate[:, LANES:], conv[:, LANES:]).astype(BF16)
    up_out[:, 2 * LANES :] = conv[:, :LANES].astype(BF16)
    up_bias = line_of(up_bias_ref)
    lines = jnp.concatenate(
        [
            up_bias[:, :HALF],
            up_bias[:, HALF:],
            line_of(gain_ref),
            line_of(bias_ref),
            line_of(conv_bias_ref),
            jnp.zeros((3, HALF), F32),
        ],
        axis=0,
    )
    lines = dot_nn(lines.astype(BF16), chosen)
    taps = dot_nn(taps_ref[...], chosen)
    for part in range(2):
        lanes = slice(part * LANES, (part + 1) * LANES)
        table_out[part, :8] = lines[:, lanes]
        table_out[part, 8 : 8 + KERNEL] = taps[:, lanes]
        table_out[part, 8 + KERNEL :] = jnp.zeros((1, LANES), F32)

    odd = lax.rem(place, 2) == 1

    def head_lanes(ref, base):
        at = pl.ds(pl.multiple_of(lax.div(place, 2) * LANES + base, LANES), LANES)
        values = ref[:, at].astype(F32)
        values = jnp.where(odd, turn(values), values)
        return jnp.where(low_lanes(values.shape[0]), values, 0.0)

    for part in range(3):
        qkv_out[:, part * LANES : (part + 1) * LANES] = head_lanes(qkv_ref, part * D).astype(BF16)
    pos_out[...] = head_lanes(pos_ref, 0).astype(BF16)
    bias_out[...] = jnp.zeros((8, LANES), F32)
    for line, ref in enumerate((content_ref, position_ref)):
        values = line_of(ref)
        picked = values[:, :LANES]
        for tile in range(1, D // LANES):
            picked = jnp.where(
                lax.div(place, 2) == tile, values[:, tile * LANES : (tile + 1) * LANES], picked
            )
        picked = jnp.where(odd, turn(picked), picked)
        bias_out[line : line + 1] = jnp.where(low_lanes(1), picked, 0.0)


def angle_rows(coarse_ref, fine_ref, block, rows):
    half = D // 2
    base = coarse_ref[pl.ds(block, 1)]
    base_sine, base_cosine = base[:, :half], base[:, half:]
    sine, cosine = fine_ref[rows, :half], fine_ref[rows, half:]
    return base_sine * cosine + base_cosine * sine, base_cosine * cosine - base_sine * sine


def item_codes(bounds_s, index):
    code = jnp.zeros_like(index)
    for item in range(1, ITEMS + 1):
        code = code + (index >= bounds_s[item]).astype(jnp.int32)
    return jnp.where(code < ITEMS, code, ITEMS + index)


def attend_kernel(
    lengths_ref,
    x_ref,
    attn_gain_ref,
    attn_bias_ref,
    mlp_gain_ref,
    mlp_bias_ref,
    qkv_ref,
    pos_ref,
    bias_ref,
    coarse_ref,
    fine_ref,
    up_ref,
    up_bias_ref,
    n_attn_out,
    n_mlp_out,
    hat_out,
    q_position_out,
    query_out,
    key_out,
    value_out,
    prob_out,
    attn_out,
    share_out,
    stats_out,
    pre_s,
    bounds_s,
):
    frames = n_attn_out.buffer.shape[0]
    half = D // 2
    fill_bounds(lengths_ref, bounds_s, frames)
    attn_gain, attn_bias = line_of(attn_gain_ref), line_of(attn_bias_ref)
    mlp_gain, mlp_bias = line_of(mlp_gain_ref), line_of(mlp_bias_ref)
    content, position = bias_ref[0:1], bias_ref[1:2]
    x_ref = x_ref()

    @pl.loop(0, frames // TALL, unroll=2)
    def _(block):
        rows = rows_of(block, TALL)
        for part in range(TALL // 32):
            at = rows_of(block, TALL, part * 32)
            at = pl.ds(pl.multiple_of(block * TALL + part * 32, 32), 32)
            hat = centre_rows(x_ref[at].astype(F32))
            hat_out.buffer[at] = hat.astype(BF16)
            n_attn_out.buffer[at] = (hat * attn_gain + attn_bias).astype(BF16)
            n_mlp_out.buffer[at] = (hat * mlp_gain + mlp_bias).astype(BF16)
        parts = dot_nn(n_attn_out.buffer[rows], qkv_ref[...])
        query = parts[:, :LANES]
        query_out.buffer[rows, :LANES] = ((query + content).astype(BF16).astype(F32) * 0.125).astype(BF16)
        q_position = (query + position).astype(BF16)
        q_position_out.buffer[rows] = q_position
        key_out.buffer[rows, :LANES] = parts[:, LANES : 2 * LANES].astype(BF16)
        value_out.buffer[rows] = parts[:, 2 * LANES :].astype(BF16)
        projected = dot_nt(q_position, pos_ref[...])
        for part in range(TALL // 32):
            at = pl.ds(pl.multiple_of(block * TALL + part * 32, 32), 32)
            inner = part * 32 % BLOCK
            sine, cosine = angle_rows(
                coarse_ref, fine_ref, block * (TALL // BLOCK) + part * 32 // BLOCK, slice(inner, inner + 32)
            )
            first = projected[part * 32 : part * 32 + 32, :half]
            second = projected[part * 32 : part * 32 + 32, half:]
            query_out.buffer[at, LANES : LANES + half] = ((first * sine + second * cosine) * 0.125).astype(BF16)
            query_out.buffer[at, LANES + half :] = ((second * sine - first * cosine) * 0.125).astype(BF16)
            key_out.buffer[at, LANES : LANES + half] = cosine.astype(BF16)
            key_out.buffer[at, LANES + half :] = sine.astype(BF16)

    for out in (n_attn_out, n_mlp_out, hat_out, q_position_out, query_out, key_out, value_out):
        out.go()
    up_ref = up_ref()
    up_bias = line_of(up_bias_ref)[:, HALF:]
    lane = lax.broadcasted_iota(jnp.int32, (16, LANES), 1)

    @pl.loop(0, frames // BLOCK)
    def _(block):
        pre_s[...] = dot_nn(n_mlp_out.buffer[rows_of(block, BLOCK)], up_ref[...])
        for part in range(BLOCK // 16):
            pre = pre_s[part * 16 : part * 16 + 16] + up_bias
            hidden = pre * normal_parts(pre)[0]
            mean = jnp.mean(hidden, axis=-1, keepdims=True)
            centred = hidden - mean
            rate = lax.rsqrt(jnp.mean(centred * centred, axis=-1, keepdims=True) + EPS)
            at = pl.ds(pl.multiple_of(block * BLOCK + part * 16, 16), 16)
            stats_out.buffer[at] = jnp.where(lane == 0, mean, rate)

    stats_out.go()
    key_code = item_codes(bounds_s, lax.broadcasted_iota(jnp.int32, (1, frames), 1))

    @pl.loop(0, frames // TALL, unroll=2)
    def _(block):
        rows = rows_of(block, TALL)
        raw = dot_nt(query_out.buffer[rows], key_out.buffer[...])
        for part in range(TALL // 32):
            start = block * TALL + part * 32
            at = pl.ds(pl.multiple_of(start, 32), 32)
            index = start + lax.broadcasted_iota(jnp.int32, (32, 1), 0)
            scaled = jnp.where(
                item_codes(bounds_s, index) == key_code, raw[part * 32 : part * 32 + 32], MASKED
            )
            weight = jnp.exp(scaled - jnp.max(scaled, axis=1, keepdims=True))
            prob_out.buffer[at] = weight.astype(BF16)
            share_out.buffer[at] = jnp.broadcast_to(1.0 / jnp.sum(weight, axis=1, keepdims=True), (32, LANES))
        attn_out.buffer[rows] = (
            dot_nn(prob_out.buffer[rows], value_out.buffer[...]) * share_out.buffer[rows]
        )


def fill_margins(wide_s, frames):
    edge = jnp.zeros((MARGIN, LANES), F32)
    wide_s[:MARGIN] = edge
    wide_s[MARGIN + frames : 2 * MARGIN + frames] = edge
    base = frames + 3 * MARGIN
    after = base + frames // 2
    low = low_lanes(MARGIN)
    wide_s[base - MARGIN : base] = jnp.where(low, 0.0, turn(wide_s[after - MARGIN : after]))
    wide_s[after : after + MARGIN] = jnp.where(low, turn(wide_s[base : base + MARGIN]), 0.0)


def item_span(bounds_s, frame):
    begin, end = bounds_s[0], bounds_s[BOUNDS - 1]
    for item in range(1, ITEMS + 1):
        edge = bounds_s[item]
        begin = jnp.where(frame >= edge, edge, begin)
    for item in range(ITEMS, 0, -1):
        edge = bounds_s[item]
        end = jnp.where(frame < edge, edge, end)
    return begin, end


def is_whole(bounds_s, start):
    begin, end = item_span(bounds_s, start)
    reach = KERNEL // 2
    low = (begin == 0) | (begin <= start - reach)
    high = (end == bounds_s[BOUNDS - 1]) | (end >= start + WINDOW + reach)
    return low & high & (end >= start + WINDOW)


def tap_limits(bounds_s, start):
    frame = start + lax.broadcasted_iota(jnp.int32, (WINDOW, LANES), 0)
    begin, end = item_span(bounds_s, frame)
    return begin - frame, end - frame


def grouped(values):
    return values.reshape(WINDOW // 8, 8, LANES)


def triple_places(step, frames):
    half = frames // 2
    return (
        pl.multiple_of(step * WINDOW, 2 * MARGIN),
        pl.multiple_of(step * WINDOW + half, 2 * MARGIN),
        pl.multiple_of(step * WINDOW + frames + 2 * MARGIN, 2 * MARGIN),
    )


def over_windows(bounds_s, frames, body):
    half = frames // 2

    @pl.loop(0, half // WINDOW)
    def _(step):
        start = step * WINDOW
        whole = is_whole(bounds_s, start) & is_whole(bounds_s, start + half)

        @pl.when(whole)
        def _():
            body(step, None)

        @pl.when(jnp.logical_not(whole))
        def _():
            first, second = tap_limits(bounds_s, start), tap_limits(bounds_s, start + half)
            low = low_lanes(WINDOW)
            rest = [jnp.where(low, one, other) for one, other in zip(first, second)]
            body(step, (first, second, rest))


def tap_view(window_ref, tap, limits):
    view = window_ref[tap + 1 : tap + 1 + WINDOW]
    if limits is not None:
        shift = tap - KERNEL // 2
        view = jnp.where((limits[0] <= shift) & (limits[1] > shift), view, 0.0)
    return grouped(view)


def mlp_first_kernel(
    lengths_ref,
    n_ref,
    up_ref,
    table_ref,
    stats_ref,
    cot_ref,
    merge_ref,
    down_ref,
    attn_ref,
    mixed_out,
    gate_pre_out,
    grad_out,
    rate_out,
    hat_out,
    early_out,
    vectors_out,
    lines_out,
    hat_s,
    slope_s,
    gate_s,
    hidden_s,
    gate_slope_s,
    conv_s,
    grad_s,
    out_s,
    back_s,
    branch_s,
    mix_s,
    taps_s,
    turn_s,
    tap_sum_s,
    columns_s,
    forward_s,
    backward_s,
    bounds_s,
):
    frames = mix_s.shape[0]
    half = frames // 2
    blocks = frames // BLOCK
    quarters, early_rows, _ = early_out.shape
    share = early_rows // 8
    channels = quarters * share
    fill_bounds(lengths_ref, bounds_s, frames)
    for part in range(2):
        for tap in range(KERNEL):
            line = jnp.broadcast_to(table_ref[part, 8 + tap : 9 + tap], (8, LANES))
            taps_s[part, tap] = line
            turn_s[part, KERNEL - 1 - tap] = line
    tap_sum_s[...] = jnp.zeros(tap_sum_s.shape, F32)
    main, rest = table_ref[0, :8], table_ref[1, :8]
    mixed_bias = jnp.where(low_lanes(1), rest[0:1], rest[1:2])
    low = low_lanes(64)
    gate_pre_ref = gate_pre_out.buffer
    n_ref = n_ref()
    stats_ref = stats_ref()

    def stat_rows(rows):
        stats = stats_ref[rows]
        return stats[:, 0:1], stats[:, 1:2]

    def chunk(start, base=0):
        return pl.ds(pl.multiple_of(start, 64) + base, 64)

    def conv_part(hidden, mean, rate, lines, rows, to_rows):
        hat = (hidden - mean) * rate
        hat_s[rows] = hat
        hat_out.buffer[rows] = hat.astype(BF16)
        conv_s[to_rows] = (hat * lines[2:3] + lines[3:4]).astype(BF16).astype(F32)

    @pl.loop(0, half // TALL)
    def _(block):
        pre = [dot_nn(n_ref[rows_of(block, TALL, base)], up_ref[...]) for base in (0, half)]
        for part in range(TALL // 64):
            inner = slice(part * 64, part * 64 + 64)
            start = block * TALL + part * 64
            mixed = []
            for values, base in zip(pre, (0, half)):
                rows = chunk(start, base)
                gate, gate_slope = gelu_parts(values[inner, :LANES] + main[0:1])
                hidden_s[rows] = gate
                gate_slope_s[rows] = gate_slope
                hidden, slope = gelu_parts(values[inner, 2 * LANES :] + main[1:2])
                mean, rate = stat_rows(rows)
                slope_s[rows] = slope * rate
                conv_part(hidden, mean, rate, main, rows, chunk(start, base + MARGIN))
                mixed.append((*gelu_parts(values[inner, LANES : 2 * LANES] + mixed_bias), mean, rate))
            (low_hidden, low_slope, low_mean, low_rate), (high_hidden, high_slope, high_mean, high_rate) = mixed
            rows = chunk(start, frames)
            hidden_s[rows] = jnp.where(low, low_hidden, turn(high_hidden))
            gate_slope_s[rows] = jnp.where(low, low_slope, turn(high_slope))
            rate = jnp.where(low, low_rate, high_rate)
            slope_s[rows] = jnp.where(low, turn(low_slope), high_slope) * rate
            conv_part(
                jnp.where(low, turn(low_hidden), high_hidden),
                jnp.where(low, low_mean, high_mean),
                rate,
                rest,
                rows,
                chunk(start, frames + 3 * MARGIN),
            )

    hat_out.go()
    fill_margins(conv_s, frames)
    tall = WINDOW + 2 * MARGIN
    outs = (0, half, frames)

    def convolve(step, limits):
        for index, base in enumerate(triple_places(step, frames)):
            forward_s[index] = conv_s[pl.ds(base, tall)]
        for index in range(3):
            own = None if limits is None else limits[index]
            total = jnp.zeros((WINDOW // 8, 8, LANES), F32)
            for tap in range(KERNEL):
                total = total + tap_view(forward_s.at[index], tap, own) * taps_s[index // 2, tap][None]
            lines = rest if index == 2 else main
            out_s[rows_of(step, WINDOW, outs[index])] = total.reshape(WINDOW, LANES) + lines[4:5]

    over_windows(bounds_s, frames, convolve)
    cot_ref = cot_ref()
    merge_ref = merge_ref()
    down_ref = down_ref()
    attn_ref = attn_ref()
    down_ref[channels:] = jnp.zeros((2 * LANES - channels, D), BF16)
    zero = jnp.zeros((8, LANES), F32)

    def branch_part(grad_gated, rows, to_rows, sums):
        up_sum, conv_sum = sums
        gate, conv = hidden_s[rows], out_s[rows]
        gate_pre = (grad_gated * conv * gate_slope_s[rows]).astype(BF16)
        gate_pre_ref[rows] = gate_pre
        grad_conv = (grad_gated * gate).astype(BF16).astype(F32)
        grad_s[to_rows] = grad_conv
        gate_pre = gate_pre.astype(F32)
        return gate * conv, gate_pre, (up_sum + fold_rows(gate_pre), conv_sum + fold_rows(grad_conv))

    def branch_step(block, sums):
        main_sums, rest_sums = sums
        grads = []
        for base in (0, half):
            rows = rows_of(block, TALL, base)
            branch = dot_nt(cot_ref[rows], merge_ref[...]).astype(BF16)
            branch_s[rows] = branch
            grads.append(dot_nt(branch, down_ref[...]))
        for part in range(TALL // 64):
            inner = slice(part * 64, part * 64 + 64)
            start = block * TALL + part * 64
            for values, base in zip(grads, (0, half)):
                rows = chunk(start, base)
                gated, gate_pre, main_sums = branch_part(
                    values[inner, :LANES], rows, chunk(start, base + MARGIN), main_sums
                )
                mix_s[rows, :LANES] = gated.astype(BF16)
                gate_s[rows, :LANES] = gate_pre.astype(BF16)
            grad = jnp.where(low, grads[0][inner, LANES:], turn(grads[1][inner, LANES:]))
            gated, gate_pre, rest_sums = branch_part(
                grad, chunk(start, frames), chunk(start, frames + 3 * MARGIN), rest_sums
            )
            low_rows, high_rows = chunk(start), chunk(start, half)
            gate_s[low_rows, LANES:] = gate_pre.astype(BF16)
            gate_s[high_rows, LANES:] = turn(gate_pre).astype(BF16)
            mix_s[low_rows, LANES:] = jnp.where(low, gated, turn(attn_ref[low_rows])).astype(BF16)
            mix_s[high_rows, LANES:] = jnp.where(low, turn(gated), turn(attn_ref[high_rows])).astype(BF16)
        return main_sums, rest_sums

    (main_up, main_conv), (rest_up, rest_conv) = lax.fori_loop(
        0, half // TALL, branch_step, ((zero, zero), (zero, zero))
    )
    gate_pre_out.go()
    fill_margins(grad_s, frames)
    ones = jnp.ones((16, frames), BF16)
    lines_out[0:1] = dot_nn(ones, branch_s[...])[0:1]
    lines_out[1:2] = dot_nn(ones, cot_ref[...])[0:1]
    lines_out[2:8] = jnp.zeros((6, D), F32)
    grad_down = dot_tn(mix_s[...], branch_s[...])
    grad_gate = dot_tn(gate_s[...], n_ref[...])
    for quarter in range(quarters):
        for tile in range(4):
            early_out[quarter, tile * share : (tile + 1) * share] = grad_down[
                quarter * share : (quarter + 1) * share, tile * LANES : (tile + 1) * LANES
            ].astype(BF16)
        early_out[quarter, 4 * share :] = grad_gate[
            :channels, quarter * LANES : (quarter + 1) * LANES
        ].astype(BF16)

    def differentiate(step, limits):
        for index, base in enumerate(triple_places(step, frames)):
            forward_s[index] = conv_s[pl.ds(base, tall)]
            backward_s[index] = grad_s[pl.ds(base, tall)]
        for index in range(3):
            own = None if limits is None else limits[index]
            total = jnp.zeros((WINDOW // 8, 8, LANES), F32)
            centre = grouped(backward_s[index, MARGIN : MARGIN + WINDOW])
            for tap in range(KERNEL):
                total = total + tap_view(backward_s.at[index], tap, own) * turn_s[index // 2, tap][None]
                tap_sum_s[index // 2, tap] += jnp.sum(tap_view(forward_s.at[index], tap, own) * centre, axis=0)
            back_s[rows_of(step, WINDOW, outs[index])] = total.reshape(WINDOW, LANES)

    over_windows(bounds_s, frames, differentiate)
    lane = lax.broadcasted_iota(jnp.int32, (64, LANES), 1)

    def norm_part(rows, lines, sums):
        gain_sum, bias_sum = sums
        back, hat, slope = back_s[rows], hat_s[rows], slope_s[rows]
        grad = back * lines[2:3]
        grad_out.buffer[rows] = (grad * slope).astype(BF16)
        rate_out.buffer[rows] = slope.astype(BF16)
        along = back * hat
        return grad, along * lines[2:3], (gain_sum + fold_rows(along), bias_sum + fold_rows(back))

    def norm_step(block, sums):
        main_sums, rest_sums = sums
        for part in range(TALL // 64):
            start = block * TALL + part * 64
            pairs = []
            for base in (0, half):
                plain, along, main_sums = norm_part(chunk(start, base), main, main_sums)
                pairs.append([plain, along])
            plain, along, rest_sums = norm_part(chunk(start, frames), rest, rest_sums)
            for item, values in enumerate((plain, along)):
                pairs[0][item] = pairs[0][item] + jnp.where(low, values, 0.0)
                pairs[1][item] = pairs[1][item] + jnp.where(low, 0.0, values)
            for (plain, along), base in zip(pairs, (0, half)):
                columns_s[chunk(start, base)] = jnp.where(
                    lane == 0,
                    jnp.sum(plain, axis=-1, keepdims=True),
                    jnp.where(lane == 1, jnp.sum(along, axis=-1, keepdims=True), 0.0),
                )
        return main_sums, rest_sums

    (main_gain, main_bias), (rest_gain, rest_bias) = lax.fori_loop(
        0, half // TALL, norm_step, ((zero, zero), (zero, zero))
    )
    grad_out.go()
    rate_out.go()
    totals = jnp.concatenate(
        [jnp.transpose(columns_s[block * BLOCK : (block + 1) * BLOCK])[:2] for block in range(blocks)], axis=0
    )
    high = totals.astype(BF16)
    low_part = (totals - high.astype(F32)).astype(BF16)
    for block in range(blocks):
        mixed_out[block, :BLOCK] = mix_s[block * BLOCK : (block + 1) * BLOCK]
        mixed_out[block, BLOCK:, :LANES] = high
        mixed_out[block, BLOCK:, LANES:] = low_part

    def vectors(part, lines):
        taps = jnp.sum(tap_sum_s[part], axis=1)[:KERNEL]
        stacked = jnp.concatenate([taps] + [one_row(line) for line in lines], axis=0)
        if part:
            stacked = stacked + turn(stacked)
        return jnp.transpose(
            jnp.concatenate([stacked, jnp.zeros((LANES - stacked.shape[0], LANES), F32)], axis=0)
        )

    vectors_out[:LANES] = vectors(0, (main_conv, main_gain, main_bias, main_up))
    vectors_out[LANES:] = vectors(1, (rest_conv, rest_gain, rest_bias, rest_up))[: channels - LANES]


def attend_back_kernel(
    cot_ref,
    merge_ref,
    head_ref,
    share_ref,
    value_ref,
    attn_ref,
    prob_ref,
    key_ref,
    coarse_ref,
    fine_ref,
    pos_ref,
    query_ref,
    n_ref,
    q_position_ref,
    qkv_ref,
    hat_ref,
    gain_ref,
    early_ref,
    branch_out,
    total_out,
    pack_out,
    lines_out,
    grad_s,
    raw_s,
    projected_s,
    parts_s,
    grads_s,
):
    place = lax.axis_index("tm")
    frames = raw_s.shape[0]
    blocks = frames // BLOCK
    half = D // 2
    zero = jnp.zeros((8, LANES), F32)
    cot_ref, merge_ref, head_ref = cot_ref(), merge_ref(), head_ref()
    head_ref[HEAD:] = jnp.zeros((LANES - HEAD, D), BF16)
    share_ref, value_ref, attn_ref = share_ref(), value_ref(), attn_ref()
    prob_ref, key_ref, pos_ref = prob_ref(), key_ref(), pos_ref()

    def score_step(block, sums):
        content_sum, position_sum = sums
        rows = rows_of(block, TALL)
        branch = dot_nt(cot_ref[rows], merge_ref[...]).astype(BF16)
        branch_out.buffer[rows] = branch
        grad = (dot_nt(branch, head_ref[...]) * share_ref[rows]).astype(BF16)
        grad_s[rows] = grad
        score = dot_nt(grad, value_ref[...])
        for part in range(TALL // 32):
            at = pl.ds(pl.multiple_of(block * TALL + part * 32, 32), 32)
            inner = slice(part * 32, part * 32 + 32)
            delta = jnp.sum(grad[inner].astype(F32) * attn_ref[at], axis=1, keepdims=True)
            raw_s[at] = (prob_ref[at].astype(F32) * (score[inner] - delta)).astype(BF16)
        query = dot_nn(raw_s[rows], key_ref[...]) * 0.125
        for part in range(TALL // 32):
            at = pl.ds(pl.multiple_of(block * TALL + part * 32, 32), 32)
            inner = part * 32 % BLOCK
            sine, cosine = angle_rows(
                coarse_ref, fine_ref, block * (TALL // BLOCK) + part * 32 // BLOCK, slice(inner, inner + 32)
            )
            inner = slice(part * 32, part * 32 + 32)
            first, second = query[inner, LANES : LANES + half], query[inner, LANES + half :]
            projected_s[at, :half] = (first * sine - second * cosine).astype(BF16)
            projected_s[at, half:] = (first * cosine + second * sine).astype(BF16)
        position = dot_nn(projected_s[rows], pos_ref[...])
        content = query[:, :LANES]
        parts_s[rows, :LANES] = (content + position).astype(BF16)
        return content_sum + fold_rows(content), position_sum + fold_rows(position)

    content_sum, position_sum = lax.fori_loop(0, frames // TALL, score_step, (zero, zero), unroll=2)
    branch_out.go()
    query_ref, n_ref, q_position_ref = query_ref(), n_ref(), q_position_ref()
    qkv_ref, hat_ref = qkv_ref(), hat_ref()
    grad_key = dot_tn(query_ref[...], raw_s[...])
    grad_value = dot_tn(grad_s[...], prob_ref[...])
    for block in range(blocks):
        at = slice(block * BLOCK, (block + 1) * BLOCK)
        parts_s[at, LANES : 2 * LANES] = jnp.transpose(grad_key[:, at]).astype(BF16)
        parts_s[at, 2 * LANES :] = jnp.transpose(grad_value[:, at]).astype(BF16)
    grads_s[:HEAD] = dot_tn(parts_s[:, :LANES], n_ref[...])[:HEAD]
    grads_s[HEAD : 2 * HEAD] = dot_nn(grad_key.astype(BF16), n_ref[...])[:HEAD]
    grads_s[2 * HEAD : 3 * HEAD] = dot_nn(grad_value.astype(BF16), n_ref[...])[:HEAD]
    grads_s[3 * HEAD :] = dot_tn(q_position_ref[...], projected_s[...])[:HEAD]
    for quarter in range(pack_out.shape[0]):
        pack_out[quarter, : 4 * HEAD] = grads_s[:, quarter * LANES : (quarter + 1) * LANES].astype(BF16)
    pack_out[:, 4 * HEAD :] = early_ref[...]
    gain = line_of(gain_ref)
    wide_zero = jnp.zeros((8, D), F32)

    def norm_step(block, sums):
        gain_sum, bias_sum = sums
        grad = dot_nt(parts_s[rows_of(block, TALL)], qkv_ref[...])
        for part in range(TALL // 32):
            at = pl.ds(pl.multiple_of(block * TALL + part * 32, 32), 32)
            own = grad[part * 32 : part * 32 + 32]
            total_out.buffer[at] = (own * gain).astype(BF16)
            gain_sum = gain_sum + fold_rows(own * hat_ref[at].astype(F32))
            bias_sum = bias_sum + fold_rows(own)
        return gain_sum, bias_sum

    gain_sum, bias_sum = lax.fori_loop(0, frames // TALL, norm_step, (wide_zero, wide_zero), unroll=2)
    lane = lax.broadcasted_iota(jnp.int32, (1, LANES), 1)

    def own_lanes(sums):
        line = one_row(sums)
        line = line + turn(line)
        tiles = [
            jnp.where(lax.div(tile * LANES + lane, HEAD) == place, line, 0.0) for tile in range(D // LANES)
        ]
        return jnp.concatenate(tiles, axis=1)

    lines_out[...] = jnp.concatenate(
        [
            one_row(gain_sum),
            one_row(bias_sum),
            own_lanes(content_sum),
            own_lanes(position_sum),
            jnp.zeros((4, D), F32),
        ],
        axis=0,
    )


def mlp_second_kernel(
    mixed_ref,
    gate_pre_ref,
    grad_ref,
    rate_ref,
    hat_ref,
    up_ref,
    norm_hat_ref,
    gain_ref,
    other_ref,
    n_ref,
    vectors_ref,
    first_lines_ref,
    head_lines_ref,
    same_out,
    apart_out,
    pack_0,
    pack_1,
    pack_2,
    pack_3,
    pre_s,
    columns_s,
    grad_up_s,
    lines_s,
    up_columns_s,
):
    packs = (pack_0, pack_1, pack_2, pack_3)
    stream = lax.axis_index("stream")
    place = lax.axis_index("tm")
    frames = pre_s.shape[0]
    half = frames // 2
    blocks = frames // BLOCK
    quarters = len(packs)
    channels = vectors_ref.shape[0]
    share = channels // quarters
    totals = jnp.zeros((2 * blocks, LANES), F32)
    for source in range(mixed_ref.shape[0]):
        both = mixed_ref[source, BLOCK:].astype(F32)
        totals = totals + (both[:, :LANES] + both[:, LANES:])
    totals = totals * (1.0 / HALF)
    columns = jnp.transpose(jnp.concatenate([totals, jnp.zeros((LANES - 2 * blocks, LANES), F32)], axis=0))
    lane = lax.broadcasted_iota(jnp.int32, (BLOCK, LANES), 1)
    for block in range(blocks):
        columns_s[block * BLOCK : (block + 1) * BLOCK] = jnp.where(
            lane == 0, columns[:, 2 * block : 2 * block + 1], columns[:, 2 * block + 1 : 2 * block + 2]
        )
    gate_pre_ref, grad_ref, rate_ref, hat_ref = gate_pre_ref(), grad_ref(), rate_ref(), hat_ref()
    up_ref, norm_hat_ref, other_ref, n_ref = up_ref(), norm_hat_ref(), other_ref(), n_ref()
    low = low_lanes(64)
    gain = line_of(gain_ref)

    def chunk(start, base=0):
        return pl.ds(pl.multiple_of(start, 64) + base, 64)

    def pre_part(rows, table, up_sum):
        plain, along = table
        hat, rate = hat_ref[rows].astype(F32), rate_ref[rows].astype(F32)
        pre = (grad_ref[rows].astype(F32) - rate * (plain + hat * along)).astype(BF16).astype(F32)
        return pre, up_sum + fold_rows(pre)

    def pre_step(block, sums):
        main_up, rest_up = sums
        for part in range(TALL // 64):
            start = block * TALL + part * 64
            tables = []
            for base in (0, half):
                rows = chunk(start, base)
                values = columns_s[rows]
                table = [values[:, item : item + 1] for item in range(2)]
                tables.append(table)
                pre, main_up = pre_part(rows, table, main_up)
                pre_s[rows, :LANES] = gate_pre_ref[rows]
                pre_s[rows, 2 * LANES :] = pre.astype(BF16)
            rows = chunk(start, frames)
            table = [jnp.where(low, one, other) for one, other in zip(*tables)]
            pre, rest_up = pre_part(rows, table, rest_up)
            gate_pre = gate_pre_ref[rows].astype(F32)
            pre_s[chunk(start), LANES : 2 * LANES] = jnp.where(low, gate_pre, turn(pre)).astype(BF16)
            pre_s[chunk(start, half), LANES : 2 * LANES] = jnp.where(low, turn(gate_pre), pre).astype(BF16)
        return main_up, rest_up

    zero = jnp.zeros((8, LANES), F32)
    main_up, rest_up = lax.fori_loop(0, half // TALL, pre_step, (zero, zero))
    grad_up_s[...] = dot_tn(pre_s[:, LANES:], n_ref[...])
    wide_zero = jnp.zeros((8, D), F32)

    def norm_step(block, sums):
        gain_sum, bias_sum = sums
        rows = rows_of(block, BLOCK)
        grad = dot_nt(pre_s[rows], up_ref[...])
        total = (grad * gain + other_ref[rows].astype(F32)).astype(BF16)
        apart = lax.bitwise_xor(block, place)
        slot = lax.div(apart, 2)

        @pl.when(lax.rem(apart, 2) == 0)
        def _():
            same_out[slot] = total

        @pl.when(lax.rem(apart, 2) == 1)
        def _():
            apart_out[slot] = total

        return gain_sum + fold_rows(grad * norm_hat_ref[rows].astype(F32)), bias_sum + fold_rows(grad)

    gain_sum, bias_sum = lax.fori_loop(0, blocks, norm_step, (wide_zero, wide_zero))
    rest_line = one_row(rest_up)
    up_columns_s[:LANES] = jnp.transpose(jnp.broadcast_to(one_row(main_up), (LANES, LANES)))
    up_columns_s[LANES:] = jnp.transpose(jnp.broadcast_to(rest_line + turn(rest_line), (LANES, LANES)))[:LOW]
    first_device = (place == 0).astype(F32)
    lines_s[...] = jnp.concatenate(
        [
            head_lines_ref[0:2],
            one_row(gain_sum),
            one_row(bias_sum),
            head_lines_ref[2:4],
            first_lines_ref[0:2] * first_device,
            jnp.zeros((8, D), F32),
        ],
        axis=0,
    )
    gate_at = KERNEL + 3
    lane = lax.broadcasted_iota(jnp.int32, (share, LANES), 1)
    for apart, pack_out in enumerate(packs):
        quarter = lax.bitwise_xor(stream, jnp.int32(apart))
        lanes = pl.ds(pl.multiple_of(quarter * LANES, LANES), LANES)
        pack_out[:LANES] = grad_up_s[LANES:, lanes].astype(BF16)
        pack_out[LANES:channels] = grad_up_s[LOW:LANES, lanes].astype(BF16)
        table = vectors_ref[pl.ds(pl.multiple_of(quarter * share, 8), share)]
        for other in range(2):
            at = pl.ds(pl.multiple_of((2 * lax.rem(quarter, 2) + other) * share, 8), share)
            column = jnp.where(
                quarter < quarters // 2, vectors_ref[at][:, gate_at : gate_at + 1], up_columns_s[at][:, 0:1]
            )
            table = jnp.where(lane == gate_at + other, column, table)
        pack_out[channels : channels + share] = table.astype(BF16)
        pack_out[channels + share :] = lines_s[:, lanes].astype(BF16)


def output_kernel(
    x_ref, mixed_ref, head_ref, down_ref, down_bias_ref, merge_ref, merge_bias_ref, out_ref, joined_out
):
    sources = mixed_ref.shape[0]
    rows = x_ref.shape[0]
    channels = HALF // sources
    share = channels // 4
    attn_parts = []
    branch_attn = jnp.zeros((rows, D), F32)
    branch_mlp = jnp.zeros((rows, D), F32)
    for source in range(sources):
        attn = turn(mixed_ref[source, :rows, LANES:].astype(F32))[:, :HEAD].astype(BF16)
        attn_parts.append(attn)
        branch_attn = branch_attn + dot_nn(attn, head_ref[source * HEAD : (source + 1) * HEAD])
        down = jnp.concatenate(
            [down_ref[(part * sources + source) * share : (part * sources + source + 1) * share] for part in range(4)],
            axis=0,
        )
        branch_mlp = branch_mlp + dot_nn(mixed_ref[source, :rows, :channels], down)
    joined = jnp.concatenate(
        [branch_attn.astype(BF16), (branch_mlp + line_of(down_bias_ref)).astype(BF16)], axis=1
    )
    result = x_ref[...].astype(F32) + dot_nn(joined, merge_ref[...]) + line_of(merge_bias_ref)
    out_ref[...] = result.astype(BF16)
    turned = jnp.transpose(joined.astype(F32))
    heads = jnp.transpose(jnp.concatenate(attn_parts, axis=1).astype(F32))
    merge_share = turned.shape[0] // (4 * sources)
    head_share = heads.shape[0] // (4 * sources)
    used = 4 * (merge_share + head_share)
    for target in range(sources):
        for part in range(4):
            at = (part * sources + target) * merge_share
            joined_out[target, part * merge_share : (part + 1) * merge_share] = turned[
                at : at + merge_share
            ].astype(BF16)
            at = (part * sources + target) * head_share
            to = 4 * merge_share + part * head_share
            joined_out[target, to : to + head_share] = heads[at : at + head_share].astype(BF16)
        joined_out[target, used:] = jnp.zeros((joined_out.shape[1] - used, rows), BF16)


def merge_kernel(joined_ref, cot_ref, branch_ref, pack_0, pack_1, pack_2, pack_3, merge_s, head_s):
    stream = lax.axis_index("stream")
    sources, _, rows = joined_ref.shape
    merge_rows = 2 * D // sources
    head_rows = D // sources
    grad_merge = jnp.zeros((merge_rows, D), F32)
    grad_head = jnp.zeros((head_rows, D), F32)
    for source in range(sources):
        at = slice(source * rows, (source + 1) * rows)
        grad_merge = grad_merge + dot_nn(joined_ref[source, :merge_rows], cot_ref[at])
        grad_head = grad_head + dot_nn(joined_ref[source, merge_rows : merge_rows + head_rows], branch_ref[at])
    merge_s[...] = grad_merge
    head_s[...] = grad_head
    for apart, pack_out in enumerate((pack_0, pack_1, pack_2, pack_3)):
        quarter = lax.bitwise_xor(stream, jnp.int32(apart))
        for grad_s, base in ((merge_s, 0), (head_s, merge_rows)):
            share = grad_s.shape[0] // 4
            at = pl.ds(pl.multiple_of(quarter * share, share), share)
            for tile in range(4):
                to = base + tile * share
                pack_out[to : to + share] = grad_s[at, tile * LANES : (tile + 1) * LANES].astype(BF16)


def pair_kernel(same_ref, other_ref, *out_refs):
    for slot, out_ref in enumerate(out_refs):
        out_ref[...] = (same_ref[slot].astype(F32) + other_ref[slot].astype(F32)).astype(BF16)


def frames_kernel(x_ref, cot_ref, *refs):
    total_refs, out_ref = refs[:-1], refs[-1]
    for part in range(x_ref.shape[0] // 32):
        rows = slice(part * 32, part * 32 + 32)
        inputs = x_ref[rows].astype(F32)
        mean = jnp.mean(inputs, axis=-1, keepdims=True)
        centred = inputs - mean
        rate = lax.rsqrt(jnp.mean(centred * centred, axis=-1, keepdims=True) + EPS)
        hat = centred * rate
        grad = total_refs[0][rows].astype(F32)
        for total_ref in total_refs[1:]:
            grad = grad + total_ref[rows].astype(F32)
        plain = jnp.mean(grad, axis=-1, keepdims=True)
        along = jnp.mean(grad * hat, axis=-1, keepdims=True)
        out_ref[rows] = cot_ref[rows].astype(F32) + rate * (grad - plain - hat * along)


def add_kernel(*refs):
    out_ref = refs[-1]
    first = 0
    for at in range(0, len(refs) - 1, 4):
        total = refs[at][...].astype(F32)
        for ref in refs[at + 1 : at + 4]:
            total = total + ref[...].astype(F32)
        out_ref[first : first + total.shape[0]] = total.astype(BF16)
        first += total.shape[0]


def early_kernel(all_ref, qkv_out, pos_out, down_out, up_out):
    sources = all_ref.shape[0]
    share = HALF // (4 * sources)

    def lines_at(base, size):
        return jnp.concatenate([all_ref[source, base : base + size] for source in range(sources)], axis=0).astype(F32)

    for kind in range(4):
        lines = jnp.transpose(lines_at(kind * HEAD, HEAD))
        if kind < 3:
            qkv_out[:, kind * D : (kind + 1) * D] = lines
        else:
            pos_out[...] = lines
    for source in range(sources):
        for tile in range(4):
            at = 4 * HEAD + tile * share
            down_out[source * share : (source + 1) * share, tile * LANES : (tile + 1) * LANES] = all_ref[
                source, at : at + share
            ].astype(F32)
    wide = sources * share
    for group in range(4):
        up_out.buffer[:, group * wide : (group + 1) * wide] = jnp.transpose(
            lines_at(4 * HEAD + 4 * share + group * share, share)
        )


def late_kernel(*refs):
    part_refs = refs[1 : HEADS + 1]
    (
        attn_gain_out,
        attn_bias_out,
        mlp_gain_out,
        mlp_bias_out,
        content_out,
        position_out,
        outw_out,
        up_out,
        up_bias_out,
        gain_out,
        bias_out,
        taps_out,
        conv_bias_out,
        down_bias_out,
        merge_out,
        merge_bias_out,
        all_s,
    ) = refs[HEADS + 1 :]
    place = lax.axis_index("tm")
    sources = all_s.shape[0]
    for apart, part_ref in enumerate(part_refs):
        all_s[lax.bitwise_xor(jnp.int32(apart), place)] = part_ref[...]
    channels = HALF // sources
    share = channels // 4

    def lines_at(base, size):
        return jnp.concatenate([all_s[source, base : base + size] for source in range(sources)], axis=0).astype(F32)

    for group in range(4):
        at = group * sources * share
        up_out.buffer[:, at : at + sources * share] = jnp.transpose(lines_at(group * share, share))
    up_out.go()
    table = jnp.transpose(lines_at(channels, share))
    taps_out[...] = table[:KERNEL]
    conv_bias_out[...] = table[KERNEL]
    gain_out[...] = table[KERNEL + 1]
    bias_out[...] = table[KERNEL + 2]
    wide = sources * share
    up_bias_out[:wide] = table[KERNEL + 3]
    up_bias_out[wide:] = table[KERNEL + 4]
    base = channels + share
    lines = all_s[0, base : base + 16].astype(F32)
    for source in range(1, sources):
        lines = lines + all_s[source, base : base + 16].astype(F32)
    outs = (attn_gain_out, attn_bias_out, mlp_gain_out, mlp_bias_out, content_out, position_out, down_bias_out, merge_bias_out)
    for line, out in enumerate(outs):
        out[...] = lines[line]
    base = base + 16
    merge_share = 2 * D // (4 * sources)
    head_share = D // (4 * sources)
    for source in range(sources):
        for tile in range(4):
            lanes = slice(tile * LANES, (tile + 1) * LANES)
            at = base + tile * merge_share
            merge_out[source * merge_share : (source + 1) * merge_share, lanes] = all_s[
                source, at : at + merge_share
            ].astype(F32)
            at = base + 4 * merge_share + tile * head_share
            outw_out[source * head_share : (source + 1) * head_share, lanes] = all_s[
                source, at : at + head_share
            ].astype(F32)


def moved(block, axis, bits):
    count = lax.axis_size(axis)
    return lax.ppermute(block, axis, [(index, index ^ bits) for index in range(count)])


def spread(block):
    near = [block] + [moved(block, "tm", bits) for bits in range(2, lax.axis_size("tm"), 2)]
    far = [moved(part, "tm", 1) for part in near]
    return [part for pair in zip(near, far) for part in pair]


def head_device(
    frames,
    lengths,
    cotangent,
    ln_attn_gain,
    ln_attn_bias,
    ln_mlp_gain,
    ln_mlp_bias,
    qkv_weight,
    content_bias,
    position_bias,
    pos_weight,
    out_weight,
    up_weight,
    up_bias,
    gate_norm_gain,
    gate_norm_bias,
    conv_kernel,
    conv_bias,
    down_weight,
    down_bias,
    merge_weight,
    merge_bias,
):
    count = lax.axis_size("tm")
    quarters = lax.axis_size("stream")
    own = frames.shape[1]
    total = own * count
    folded = total + total // 2
    padded = folded + 4 * MARGIN
    share = HALF // (quarters * count)
    channels = HALF // count
    quarter = D // quarters
    own_frames = frames[0]
    own_cotangent = cotangent[0]

    whole = Part()
    blocks = spread(own_frames)
    cot = lax.all_gather(own_cotangent, "tm", axis=0, tiled=True)
    up_own, table, qkv_own, pos_own, bias_own = kernel_call(
        select_kernel,
        [
            ((D, 3 * LANES), BF16),
            ((2, 8 + KERNEL + 1, LANES), F32),
            ((D, 3 * LANES), BF16),
            ((D, LANES), BF16),
            ((8, LANES), F32),
        ],
        10 * "v",
        micros=4,
    )(
        up_weight,
        up_bias,
        gate_norm_gain,
        gate_norm_bias,
        conv_bias,
        conv_kernel,
        qkv_weight,
        pos_weight,
        content_bias,
        position_bias,
    )
    frequency = jnp.exp(jnp.arange(D // 2, dtype=F32) * (-2.0 * math.log(10000.0) / D))
    coarse = jnp.arange(0, total, BLOCK, dtype=F32)[:, None] * frequency[None]
    fine = jnp.arange(BLOCK, dtype=F32)[:, None] * frequency[None]
    coarse_table = jnp.concatenate([jnp.sin(coarse), jnp.cos(coarse)], axis=1)
    fine_table = jnp.concatenate([jnp.sin(fine), jnp.cos(fine)], axis=1)

    n_attn, n_mlp, hat, q_position, query, key, value, prob, attn, row_share, stats = kernel_call(
        attend_kernel,
        [
            ((total, D), BF16, 1),
            ((total, D), BF16, 1),
            ((total, D), BF16, 1),
            ((total, LANES), BF16, 1),
            ((total, LANES + D), BF16, 1),
            ((total, LANES + D), BF16, 1),
            ((total, LANES), BF16, 1),
            ((total, total), BF16, 1),
            ((total, LANES), F32, 1),
            ((total, LANES), F32, 1),
            ((total, LANES), F32, 1),
        ],
        [
            "s",
            blocks_part(),
            *"vvvvvvvvv",
            Part((D, HALF), lambda refs, buffer: [(refs[0].at[:, pl.ds(HALF, HALF)], buffer)]),
            "v",
        ],
        [((BLOCK, HALF), F32)],
        bounds=True,
        micros=18,
    )(
        lengths,
        *blocks,
        ln_attn_gain,
        ln_attn_bias,
        ln_mlp_gain,
        ln_mlp_bias,
        qkv_own,
        pos_own,
        bias_own,
        coarse_table,
        fine_table,
        up_weight,
        up_bias,
    )

    def own_down(refs, buffer):
        place = lax.axis_index("tm")
        stride = HALF // quarters
        return [
            (
                refs[0].at[pl.ds(pl.multiple_of(part * stride + share * place, 16), share)],
                buffer.at[pl.ds(part * share, share)],
            )
            for part in range(quarters)
        ]

    mixed, gate_pre, grad_y, slope, gate_hat, early_pack, vectors, first_lines = kernel_call(
        mlp_first_kernel,
        [
            ((count, own + 16, 2 * LANES), BF16),
            ((folded, LANES), BF16, 1),
            ((folded, LANES), BF16, 1),
            ((folded, LANES), BF16, 1),
            ((folded, LANES), BF16, 1),
            ((quarters, 8 * share, LANES), BF16),
            ((channels, LANES), F32),
            ((8, D), F32),
        ],
        [
            "s",
            whole,
            "v",
            "v",
            whole,
            whole,
            rows_part(D, D),
            Part((2 * LANES, D), own_down),
            whole,
        ],
        [
            ((folded, LANES), F32),
            ((folded, LANES), F32),
            ((total, 2 * LANES), BF16),
            ((folded, LANES), F32),
            ((folded, LANES), F32),
            ((padded, LANES), F32),
            ((padded, LANES), F32),
            ((folded, LANES), F32),
            ((folded, LANES), F32),
            ((total, D), BF16),
            ((total, 2 * LANES), BF16),
            ((2, 32, 8, LANES), F32),
            ((2, 32, 8, LANES), F32),
            ((2, 32, 8, LANES), F32),
            ((total, LANES), F32),
            ((3, WINDOW + 2 * MARGIN, LANES), F32),
            ((3, WINDOW + 2 * MARGIN, LANES), F32),
        ],
        bounds=True,
        micros=20,
    )(lengths, n_mlp, up_own, table, stats, cot, merge_weight, down_weight, attn)
    mixed_own = lax.all_to_all(mixed, "tm", 0, 0, tiled=True)

    def own_head(refs, buffer):
        at = pl.ds(pl.multiple_of(lax.axis_index("tm") * HEAD, HEAD), HEAD)
        return [(refs[0].at[at], buffer.at[pl.ds(0, HEAD)])]

    branch, from_attn, head_pack, head_lines = kernel_call(
        attend_back_kernel,
        [
            ((total, D), BF16, 1),
            ((total, D), BF16, 1),
            ((quarters, 4 * HEAD + 8 * share, LANES), BF16),
            ((8, D), F32),
        ],
        [
            whole,
            rows_part(0, D),
            Part((LANES, D), own_head),
            whole,
            whole,
            whole,
            whole,
            whole,
            "v",
            "v",
            whole,
            Part((total, LANES), lambda refs, buffer: [(refs[0].at[:, pl.ds(0, LANES)], buffer)]),
            whole,
            whole,
            whole,
            whole,
            "v",
            "v",
        ],
        [
            ((total, LANES), BF16),
            ((total, total), BF16),
            ((total, D), BF16),
            ((total, 3 * LANES), BF16),
            ((4 * HEAD, D), F32),
        ],
        micros=14,
    )(
        cot,
        merge_weight,
        out_weight,
        row_share,
        value,
        attn,
        prob,
        key,
        coarse_table,
        fine_table,
        pos_own,
        query,
        n_attn,
        q_position,
        qkv_own,
        hat,
        ln_attn_gain,
        early_pack,
    )
    head_part = lax.psum_scatter(head_pack, "stream", scatter_dimension=0)
    head_all = lax.all_gather(head_part, "tm", axis=0)

    out_rows, joined = kernel_call(
        output_kernel,
        [((own, D), BF16), ((count, 256, own), BF16)],
        "vvvvvvv",
        micros=3,
        megas=24,
    )(own_frames, mixed_own, out_weight, down_weight, down_bias, merge_weight, merge_bias)
    joined_all = lax.all_to_all(joined, "tm", 0, 0, tiled=True)

    pack_rows = 5 * share + 16
    same, apart, *up_packs = kernel_call(
        mlp_second_kernel,
        [((count // 2, own, D), BF16)] * 2 + [((pack_rows, LANES), BF16)] * quarters,
        ["v", *([whole] * 6), "v", whole, whole, *"vvv"],
        [
            ((total, 3 * LANES), BF16),
            ((total, LANES), F32),
            ((2 * LANES, D), F32),
            ((16, D), F32),
            ((channels, LANES), F32),
        ],
        micros=10,
    )(
        mixed_own,
        gate_pre,
        grad_y,
        slope,
        gate_hat,
        up_own,
        hat,
        ln_mlp_gain,
        from_attn,
        n_mlp,
        vectors,
        first_lines,
        head_lines,
    )
    sibling = moved(apart, "tm", 1)
    up_parts = [up_packs[0]] + [moved(up_packs[bits], "stream", bits) for bits in range(1, quarters)]
    pairs = kernel_call(pair_kernel, [((own, D), BF16)] * (count // 2), "vv", micros=1, megas=24)(same, sibling)
    sums = [pairs[0]] + [moved(pairs[slot], "tm", 2 * slot) for slot in range(1, count // 2)]
    joined_all, _ = lax.optimization_barrier((joined_all, pairs[0]))
    merge_rows = 3 * D // count
    merge_packs = kernel_call(
        merge_kernel,
        [((merge_rows, LANES), BF16)] * quarters,
        "vvv",
        [((2 * D // count, D), F32), ((D // count, D), F32)],
        micros=2,
        megas=24,
    )(joined_all, cot, branch)
    merge_parts = [merge_packs[0]] + [moved(merge_packs[bits], "stream", bits) for bits in range(1, quarters)]
    (late_part,) = kernel_call(
        add_kernel, [((pack_rows + merge_rows, LANES), BF16)], 2 * quarters * "v", micros=1, megas=24
    )(*up_parts, *merge_parts)
    late_parts = spread(late_part)
    (grad_frames,) = kernel_call(frames_kernel, [((own, D), F32)], (2 + count // 2) * "v", micros=1, megas=24)(
        own_frames, own_cotangent, *sums
    )
    grad_qkv, grad_pos, grad_down, half_up = kernel_call(
        early_kernel,
        [
            ((quarter, 3 * D), F32),
            ((quarter, D), F32),
            ((HALF // quarters, D), F32),
            ((quarter, 2 * HALF), F32, 1, (quarter, HALF), lambda ref: ref.at[:, pl.ds(0, HALF)]),
        ],
        "v",
        micros=2,
        megas=24,
    )(head_all)
    late = kernel_call(
        late_kernel,
        [((quarter,), F32)] * 6
        + [
            ((quarter, D), F32),
            ((quarter, 2 * HALF), F32, 1, (quarter, HALF), lambda ref: ref.at[:, pl.ds(HALF, HALF)]),
            ((2 * HALF // quarters,), F32),
            ((HALF // quarters,), F32),
            ((HALF // quarters,), F32),
            ((KERNEL, HALF // quarters), F32),
            ((HALF // quarters,), F32),
            ((quarter,), F32),
            ((2 * D // quarters, D), F32),
            ((quarter,), F32),
        ],
        "k" + count * "v",
        [((count,) + late_part.shape, BF16)],
        micros=2,
        megas=24,
        aliases={0: 7},
    )(half_up, *late_parts)
    return (
        (out_rows[None], grad_frames[None])
        + tuple(late[:4])
        + (grad_qkv,)
        + tuple(late[4:6])
        + (grad_pos,)
        + tuple(late[6:13])
        + (grad_down,)
        + tuple(late[13:])
    )


def per_device(*operands):
    fits = (
        lax.axis_size("tm") == HEADS
        and lax.axis_size("stream") * LANES == D
        and operands[0].shape[1] == BLOCK
    )
    return head_device(*operands) if fits else frame_device(*operands)


def solution(mesh):
    return jax.shard_map(
        per_device,
        mesh=mesh,
        in_specs=(
            P("stream", "tm", None),
            P("stream", None),
            P("stream", "tm", None),
            P(),
            P(),
            P(),
            P(),
            P(),
            P(),
            P(),
            P(),
            P(),
            P(),
            P(),
            P(),
            P(),
            P(),
            P(),
            P(),
            P(),
            P(),
            P(),
        ),
        out_specs=(
            P("stream", "tm", None),
            P("stream", "tm", None),
            P("stream"),
            P("stream"),
            P("stream"),
            P("stream"),
            P("stream", None),
            P("stream"),
            P("stream"),
            P("stream", None),
            P("stream", None),
            P("stream", None),
            P("stream"),
            P("stream"),
            P("stream"),
            P(None, "stream"),
            P("stream"),
            P("stream", None),
            P("stream"),
            P("stream", None),
            P("stream"),
        ),
        check_vma=False,
    )
```

```python
import math

import jax
import jax.numpy as jnp
from jax import lax
from jax.experimental import pallas as pl
from jax.experimental.pallas import tpu as pltpu
from jax.sharding import PartitionSpec as P

D = 512
HEADS = 8
HEAD = 64
KERNEL = 31
ITEMS = 5
HALF = 1536


EPS = 1e-05
MASKED = -1e30


def extended(block, sides, width):
    for axis, dim in sides:
        count = lax.axis_size(axis)
        forward = [(i, i + 1) for i in range(count - 1)]
        backward = [(target, source) for source, target in forward]
        low = lax.ppermute(
            lax.slice_in_dim(block, block.shape[dim] - width, None, axis=dim), axis, forward
        )
        high = lax.ppermute(lax.slice_in_dim(block, 0, width, axis=dim), axis, backward)
        block = jnp.concatenate([low, block, high], axis=dim)
    return block


def norm_rows(inputs, scale_row, shift_row):
    row_mean = jnp.mean(inputs, axis=-1, keepdims=True)
    centred = inputs - row_mean
    spread = jnp.mean(centred * centred, axis=-1, keepdims=True)
    return centred * lax.rsqrt(spread + EPS) * scale_row + shift_row


def gelu_exact(inputs):
    return jax.nn.gelu(inputs, approximate=False)


def frame_info(lengths, offset, extent):
    item_ends = jnp.cumsum(lengths)
    first_table = jnp.concatenate([item_ends - lengths, item_ends[-1:]])
    frame_index = offset + jnp.arange(extent, dtype=jnp.int32)
    item_of = jnp.sum((frame_index[:, None] >= item_ends[None, :]).astype(jnp.int32), axis=1)
    labels = jnp.arange(ITEMS + 1, dtype=jnp.int32)
    first_frame = jnp.sum(
        jnp.where(item_of[:, None] == labels[None, :], first_table[None, :], 0), axis=1
    )
    return (frame_index, item_of, frame_index - first_frame)


def angles(place_in):
    frequency = jnp.exp(jnp.arange(D // 2, dtype=jnp.float32) * (-2.0 * math.log(10000.0) / D))
    phase_angle = place_in.astype(jnp.float32)[:, None] * frequency[None, :]
    return (jnp.sin(phase_angle), jnp.cos(phase_angle))


def rel_query(projected, sine_rows, cosine_rows):
    half_size = projected.shape[-1] // 2
    first_half = projected[..., :half_size]
    second_half = projected[..., half_size:]
    sine_wide = sine_rows[:, None, :]
    cosine_wide = cosine_rows[:, None, :]
    return jnp.concatenate(
        [
            first_half * sine_wide + second_half * cosine_wide,
            second_half * sine_wide - first_half * cosine_wide,
        ],
        axis=-1,
    )


def step_size(extent):
    return math.gcd(extent, 512)


def score_block(q_content, q_rel, query_item, query_frame, key_block, key_start, lengths):
    extent = key_block.shape[0]
    key_frame, key_item, key_place = frame_info(lengths, key_start, extent)
    sine_rows, cosine_rows = angles(key_place)
    k_rel = jnp.concatenate([cosine_rows, sine_rows], axis=1).astype(jnp.bfloat16)
    raw_scores = jnp.einsum(
        "qhe,khe->hqk",
        q_content,
        key_block.reshape(extent, HEADS, HEAD),
        preferred_element_type=jnp.float32,
    )
    raw_scores = raw_scores + jnp.einsum(
        "qhc,kc->hqk", q_rel, k_rel, preferred_element_type=jnp.float32
    )
    allowed = (query_item[:, None] == key_item[None, :]) & (
        (query_item[:, None] < ITEMS) | (query_frame[:, None] == key_frame[None, :])
    )
    return (raw_scores, allowed, k_rel)


def block_grads(
    q_content,
    q_rel,
    query_item,
    query_frame,
    grad_out,
    log_total,
    delta_rows,
    key_block,
    value_block,
    key_start,
    lengths,
):
    extent = key_block.shape[0]
    raw_scores, allowed, k_rel = score_block(
        q_content, q_rel, query_item, query_frame, key_block, key_start, lengths
    )
    prob_rows = jnp.where(allowed[None], jnp.exp(raw_scores * 0.125 - log_total[:, :, None]), 0.0)
    grad_prob = jnp.einsum(
        "qhe,khe->hqk",
        grad_out,
        value_block.reshape(extent, HEADS, HEAD),
        preferred_element_type=jnp.float32,
    )
    grad_raw = (prob_rows * (grad_prob - delta_rows[:, :, None]) * 0.125).astype(jnp.bfloat16)
    return (prob_rows.astype(jnp.bfloat16), grad_raw, k_rel)


def frame_device(
    frames,
    lengths,
    cotangent,
    ln_attn_gain,
    ln_attn_bias,
    ln_mlp_gain,
    ln_mlp_bias,
    qkv_weight,
    content_bias,
    position_bias,
    pos_weight,
    out_weight,
    up_weight,
    up_bias,
    gate_norm_gain,
    gate_norm_bias,
    conv_kernel,
    conv_bias,
    down_weight,
    down_bias,
    merge_weight,
    merge_bias,
):
    row_count = frames.shape[1]
    cycle_size = lax.axis_size("tm")
    offset = lax.axis_index("tm") * row_count
    stream_lengths = lengths[0]
    inputs = frames[0].astype(jnp.float32)
    frame_index, item_of, place_in = frame_info(stream_lengths, offset, row_count)
    sine_rows, cosine_rows = angles(place_in)
    attn_norm, attn_pull = jax.vjp(
        norm_rows, inputs, ln_attn_gain.astype(jnp.float32), ln_attn_bias.astype(jnp.float32)
    )
    mlp_norm, mlp_pull = jax.vjp(
        norm_rows, inputs, ln_mlp_gain.astype(jnp.float32), ln_mlp_bias.astype(jnp.float32)
    )
    attn_norm_low = attn_norm.astype(jnp.bfloat16)
    mlp_norm_low = mlp_norm.astype(jnp.bfloat16)
    qkv_rows = jnp.dot(attn_norm_low, qkv_weight, preferred_element_type=jnp.float32)
    query_rows = qkv_rows[:, :D]
    key_rows = qkv_rows[:, D : 2 * D].astype(jnp.bfloat16)
    value_rows = qkv_rows[:, 2 * D :].astype(jnp.bfloat16)
    q_content = (query_rows + content_bias.astype(jnp.float32)).astype(jnp.bfloat16)
    q_position = (query_rows + position_bias.astype(jnp.float32)).astype(jnp.bfloat16)
    content_heads = q_content.reshape(row_count, HEADS, HEAD)
    position_heads = q_position.reshape(row_count, HEADS, HEAD)
    pos_heads = pos_weight.reshape(D, HEADS, HEAD)
    projected = jnp.einsum(
        "the,che->thc", position_heads, pos_heads, preferred_element_type=jnp.float32
    )
    q_rel = rel_query(projected, sine_rows, cosine_rows).astype(jnp.bfloat16)
    start_state = (
        jnp.full((HEADS, row_count), MASKED, jnp.float32),
        jnp.zeros((HEADS, row_count), jnp.float32),
        jnp.zeros((HEADS, row_count, HEAD), jnp.float32),
    )
    fold_state = start_state
    key_piece = lax.all_gather(key_rows, "tm", axis=0, tiled=True)
    value_piece = lax.all_gather(value_rows, "tm", axis=0, tiled=True)
    extent = key_piece.shape[0]
    step_rows = step_size(extent)

    def forward_one_step(inner_state, step_index):
        row_top, row_total, row_acc = inner_state
        key_block = lax.dynamic_slice_in_dim(key_piece, step_index * step_rows, step_rows, 0)
        value_block = lax.dynamic_slice_in_dim(value_piece, step_index * step_rows, step_rows, 0)
        raw_scores, allowed, k_rel = score_block(
            content_heads,
            q_rel,
            item_of,
            frame_index,
            key_block,
            step_index * step_rows,
            stream_lengths,
        )
        scaled = jnp.where(allowed[None], raw_scores * 0.125, MASKED)
        new_top = jnp.maximum(row_top, jnp.max(scaled, axis=2))
        weight = jnp.where(allowed[None], jnp.exp(scaled - new_top[:, :, None]), 0.0)
        factor = jnp.exp(row_top - new_top)
        row_total = row_total * factor + jnp.sum(weight, axis=2)
        row_acc = row_acc * factor[:, :, None] + jnp.einsum(
            "hqk,khe->hqe",
            weight.astype(jnp.bfloat16),
            value_block.reshape(step_rows, HEADS, HEAD),
            preferred_element_type=jnp.float32,
        )
        return ((new_top, row_total, row_acc), None)

    fold_state, unused = lax.scan(
        forward_one_step, fold_state, jnp.arange(extent // step_rows, dtype=jnp.int32)
    )
    row_top, row_total, row_acc = fold_state
    attn_heads = row_acc / row_total[:, :, None]
    log_total = row_top + jnp.log(row_total)
    attn_low = jnp.transpose(attn_heads, (1, 0, 2)).reshape(row_count, D).astype(jnp.bfloat16)
    branch_attn = jnp.dot(attn_low, out_weight, preferred_element_type=jnp.float32).astype(
        jnp.bfloat16
    )
    hidden_pre = jnp.dot(
        mlp_norm_low, up_weight, preferred_element_type=jnp.float32
    ) + up_bias.astype(jnp.float32)
    hidden, gelu_pull = jax.vjp(gelu_exact, hidden_pre)
    gate_half = hidden[:, :HALF]
    conv_norm, conv_pull = jax.vjp(
        norm_rows,
        hidden[:, HALF:],
        gate_norm_gain.astype(jnp.float32),
        gate_norm_bias.astype(jnp.float32),
    )
    conv_in = conv_norm.astype(jnp.bfloat16)
    half_width = KERNEL // 2
    conv_wide = extended(conv_in, (("tm", 0),), half_width)
    wide_frame, wide_item, wide_place = frame_info(
        stream_lengths, offset - half_width, row_count + 2 * half_width
    )
    kernel_rows = conv_kernel.astype(jnp.float32)
    conv_out = conv_bias.astype(jnp.float32) + jnp.zeros_like(gate_half)
    for tap_index in range(KERNEL):
        same_item = (wide_item[tap_index : tap_index + row_count] == item_of)[:, None]
        conv_out = (
            conv_out
            + jnp.where(
                same_item, conv_wide[tap_index : tap_index + row_count].astype(jnp.float32), 0.0
            )
            * kernel_rows[tap_index]
        )
    gated_low = (gate_half * conv_out).astype(jnp.bfloat16)
    branch_mlp = (
        jnp.dot(gated_low, down_weight, preferred_element_type=jnp.float32)
        + down_bias.astype(jnp.float32)
    ).astype(jnp.bfloat16)
    joined = jnp.concatenate([branch_attn, branch_mlp], axis=1)
    result = (
        inputs
        + jnp.dot(joined, merge_weight, preferred_element_type=jnp.float32)
        + merge_bias.astype(jnp.float32)
    )
    out_rows = result.astype(jnp.bfloat16)[None]
    grad_low = cotangent[0]
    grad_rows = grad_low.astype(jnp.float32)
    grad_merge_bias = jnp.sum(grad_rows, axis=0)
    grad_merge_weight = jnp.einsum(
        "tc,td->cd", joined, grad_low, preferred_element_type=jnp.float32
    )
    grad_joined = jnp.einsum(
        "td,cd->tc", grad_low, merge_weight, preferred_element_type=jnp.float32
    )
    grad_attn_branch = grad_joined[:, :D].astype(jnp.bfloat16)
    grad_mlp_branch = grad_joined[:, D:].astype(jnp.bfloat16)
    grad_down_weight = jnp.einsum(
        "tc,td->cd", gated_low, grad_mlp_branch, preferred_element_type=jnp.float32
    )
    grad_down_bias = jnp.sum(grad_mlp_branch.astype(jnp.float32), axis=0)
    grad_gated = jnp.einsum(
        "td,cd->tc", grad_mlp_branch, down_weight, preferred_element_type=jnp.float32
    )
    grad_gate_half = grad_gated * conv_out
    grad_conv_out = (grad_gated * gate_half).astype(jnp.bfloat16)
    grad_conv_rows = grad_conv_out.astype(jnp.float32)
    grad_conv_bias = jnp.sum(grad_conv_rows, axis=0)
    grad_wide = extended(grad_conv_out, (("tm", 0),), half_width)
    kernel_list = []
    grad_conv_in = jnp.zeros_like(grad_conv_rows)
    for tap_index in range(KERNEL):
        same_item = (wide_item[tap_index : tap_index + row_count] == item_of)[:, None]
        kernel_list.append(
            jnp.sum(
                jnp.where(
                    same_item, conv_wide[tap_index : tap_index + row_count].astype(jnp.float32), 0.0
                )
                * grad_conv_rows,
                axis=0,
            )
        )
        back_start = 2 * half_width - tap_index
        back_item = (wide_item[back_start : back_start + row_count] == item_of)[:, None]
        grad_conv_in = (
            grad_conv_in
            + jnp.where(
                back_item, grad_wide[back_start : back_start + row_count].astype(jnp.float32), 0.0
            )
            * kernel_rows[tap_index]
        )
    grad_conv_kernel = jnp.stack(kernel_list)
    grad_second, grad_gate_norm_gain, grad_gate_norm_bias = conv_pull(grad_conv_in)
    (grad_pre_rows,) = gelu_pull(jnp.concatenate([grad_gate_half, grad_second], axis=1))
    grad_pre = grad_pre_rows.astype(jnp.bfloat16)
    grad_up_bias = jnp.sum(grad_pre.astype(jnp.float32), axis=0)
    grad_up_weight = jnp.einsum(
        "tc,tf->cf", mlp_norm_low, grad_pre, preferred_element_type=jnp.float32
    )
    grad_mlp_norm = jnp.einsum("tf,cf->tc", grad_pre, up_weight, preferred_element_type=jnp.float32)
    grad_out_weight = jnp.einsum(
        "tc,td->cd", attn_low, grad_attn_branch, preferred_element_type=jnp.float32
    )
    grad_attn_low = jnp.einsum(
        "td,cd->tc", grad_attn_branch, out_weight, preferred_element_type=jnp.float32
    ).astype(jnp.bfloat16)
    grad_out_heads = grad_attn_low.reshape(row_count, HEADS, HEAD)
    delta_rows = jnp.sum(
        jnp.transpose(grad_out_heads.astype(jnp.float32), (1, 0, 2)) * attn_heads, axis=2
    )
    total_frames = row_count * cycle_size
    back_start_state = (
        jnp.zeros((row_count, HEADS, HEAD), jnp.float32),
        jnp.zeros((row_count, HEADS, D), jnp.float32),
        jnp.zeros((total_frames, D), jnp.float32),
        jnp.zeros((total_frames, D), jnp.float32),
    )
    back_key_piece = lax.all_gather(key_rows, "tm", axis=0, tiled=True)
    back_value_piece = lax.all_gather(value_rows, "tm", axis=0, tiled=True)
    extent = back_key_piece.shape[0]
    back_step_rows = step_size(extent)

    def back_one_step(inner_state, step_index):
        grad_content, grad_rel = inner_state
        key_block = lax.dynamic_slice_in_dim(
            back_key_piece, step_index * back_step_rows, back_step_rows, 0
        )
        value_block = lax.dynamic_slice_in_dim(
            back_value_piece, step_index * back_step_rows, back_step_rows, 0
        )
        prob_low, grad_raw, k_rel = block_grads(
            content_heads,
            q_rel,
            item_of,
            frame_index,
            grad_out_heads,
            log_total,
            delta_rows,
            key_block,
            value_block,
            step_index * back_step_rows,
            stream_lengths,
        )
        grad_content = grad_content + jnp.einsum(
            "hqk,khe->qhe",
            grad_raw,
            key_block.reshape(back_step_rows, HEADS, HEAD),
            preferred_element_type=jnp.float32,
        )
        grad_rel = grad_rel + jnp.einsum(
            "hqk,kc->qhc", grad_raw, k_rel, preferred_element_type=jnp.float32
        )
        key_part = jnp.einsum(
            "hqk,qhe->khe", grad_raw, content_heads, preferred_element_type=jnp.float32
        ).reshape(back_step_rows, D)
        value_part = jnp.einsum(
            "hqk,qhe->khe", prob_low, grad_out_heads, preferred_element_type=jnp.float32
        ).reshape(back_step_rows, D)
        return ((grad_content, grad_rel), (key_part, value_part))

    inner_state, block_parts = lax.scan(
        back_one_step,
        (back_start_state[0], back_start_state[1]),
        jnp.arange(extent // back_step_rows, dtype=jnp.int32),
    )
    key_all = block_parts[0].reshape(extent, D)
    value_all = block_parts[1].reshape(extent, D)
    grad_content, grad_rel, key_all, value_all = (
        inner_state[0],
        inner_state[1],
        key_all,
        value_all,
    )
    grad_keys, grad_values = (
        lax.psum_scatter(key_all, "tm", scatter_dimension=0, tiled=True),
        lax.psum_scatter(value_all, "tm", scatter_dimension=0, tiled=True),
    )
    half_size = D // 2
    rel_first = grad_rel[..., :half_size]
    rel_second = grad_rel[..., half_size:]
    sine_wide = sine_rows[:, None, :]
    cosine_wide = cosine_rows[:, None, :]
    grad_projected = jnp.concatenate(
        [
            rel_first * sine_wide - rel_second * cosine_wide,
            rel_first * cosine_wide + rel_second * sine_wide,
        ],
        axis=-1,
    ).astype(jnp.bfloat16)
    grad_pos_weight = jnp.einsum(
        "thc,the->che", grad_projected, position_heads, preferred_element_type=jnp.float32
    ).reshape(D, D)
    grad_q_position = jnp.einsum(
        "thc,che->the", grad_projected, pos_heads, preferred_element_type=jnp.float32
    )
    grad_content_bias = jnp.sum(grad_content, axis=0).reshape(D)
    grad_position_bias = jnp.sum(grad_q_position, axis=0).reshape(D)
    grad_query = (grad_content + grad_q_position).reshape(row_count, D).astype(jnp.bfloat16)
    grad_qkv = jnp.concatenate(
        [grad_query, grad_keys.astype(jnp.bfloat16), grad_values.astype(jnp.bfloat16)], axis=1
    )
    grad_qkv_weight = jnp.einsum(
        "tc,tf->cf", attn_norm_low, grad_qkv, preferred_element_type=jnp.float32
    )
    grad_attn_norm = jnp.einsum(
        "tf,cf->tc", grad_qkv, qkv_weight, preferred_element_type=jnp.float32
    )
    grad_from_attn, grad_ln_attn_gain, grad_ln_attn_bias = attn_pull(grad_attn_norm)
    grad_from_mlp, grad_ln_mlp_gain, grad_ln_mlp_bias = mlp_pull(grad_mlp_norm)
    grad_inputs = grad_rows + grad_from_attn + grad_from_mlp
    weight_grads = (
        grad_ln_attn_gain,
        grad_ln_attn_bias,
        grad_ln_mlp_gain,
        grad_ln_mlp_bias,
        grad_qkv_weight,
        grad_content_bias,
        grad_position_bias,
        grad_pos_weight,
        grad_out_weight,
        grad_up_weight,
        grad_up_bias,
        grad_gate_norm_gain,
        grad_gate_norm_bias,
        grad_conv_kernel,
        grad_conv_bias,
        grad_down_weight,
        grad_down_bias,
        grad_merge_weight,
        grad_merge_bias,
    )
    summed = lax.psum(
        (
            weight_grads[0],
            weight_grads[1],
            weight_grads[2],
            weight_grads[3],
            weight_grads[4],
            weight_grads[5],
            weight_grads[6],
            weight_grads[7],
            weight_grads[8],
            weight_grads[9],
            weight_grads[10],
            weight_grads[11],
            weight_grads[12],
            weight_grads[13],
            weight_grads[14],
            weight_grads[15],
            weight_grads[16],
            weight_grads[17],
            weight_grads[18],
        ),
        "tm",
    )
    shares = (
        lax.psum_scatter(
            summed[0].astype(jnp.bfloat16), "stream", scatter_dimension=0, tiled=True
        ).astype(jnp.float32),
        lax.psum_scatter(
            summed[1].astype(jnp.bfloat16), "stream", scatter_dimension=0, tiled=True
        ).astype(jnp.float32),
        lax.psum_scatter(
            summed[2].astype(jnp.bfloat16), "stream", scatter_dimension=0, tiled=True
        ).astype(jnp.float32),
        lax.psum_scatter(
            summed[3].astype(jnp.bfloat16), "stream", scatter_dimension=0, tiled=True
        ).astype(jnp.float32),
        lax.psum_scatter(
            summed[4].astype(jnp.bfloat16), "stream", scatter_dimension=0, tiled=True
        ).astype(jnp.float32),
        lax.psum_scatter(
            summed[5].astype(jnp.bfloat16), "stream", scatter_dimension=0, tiled=True
        ).astype(jnp.float32),
        lax.psum_scatter(
            summed[6].astype(jnp.bfloat16), "stream", scatter_dimension=0, tiled=True
        ).astype(jnp.float32),
        lax.psum_scatter(
            summed[7].astype(jnp.bfloat16), "stream", scatter_dimension=0, tiled=True
        ).astype(jnp.float32),
        lax.psum_scatter(
            summed[8].astype(jnp.bfloat16), "stream", scatter_dimension=0, tiled=True
        ).astype(jnp.float32),
        lax.psum_scatter(
            summed[9].astype(jnp.bfloat16), "stream", scatter_dimension=0, tiled=True
        ).astype(jnp.float32),
        lax.psum_scatter(
            summed[10].astype(jnp.bfloat16), "stream", scatter_dimension=0, tiled=True
        ).astype(jnp.float32),
        lax.psum_scatter(
            summed[11].astype(jnp.bfloat16), "stream", scatter_dimension=0, tiled=True
        ).astype(jnp.float32),
        lax.psum_scatter(
            summed[12].astype(jnp.bfloat16), "stream", scatter_dimension=0, tiled=True
        ).astype(jnp.float32),
        lax.psum_scatter(
            summed[13].astype(jnp.bfloat16), "stream", scatter_dimension=1, tiled=True
        ).astype(jnp.float32),
        lax.psum_scatter(
            summed[14].astype(jnp.bfloat16), "stream", scatter_dimension=0, tiled=True
        ).astype(jnp.float32),
        lax.psum_scatter(
            summed[15].astype(jnp.bfloat16), "stream", scatter_dimension=0, tiled=True
        ).astype(jnp.float32),
        lax.psum_scatter(
            summed[16].astype(jnp.bfloat16), "stream", scatter_dimension=0, tiled=True
        ).astype(jnp.float32),
        lax.psum_scatter(
            summed[17].astype(jnp.bfloat16), "stream", scatter_dimension=0, tiled=True
        ).astype(jnp.float32),
        lax.psum_scatter(
            summed[18].astype(jnp.bfloat16), "stream", scatter_dimension=0, tiled=True
        ).astype(jnp.float32),
    )
    return (out_rows, grad_inputs[None]) + tuple(shares)


LANES = 128
LOW = LANES // 2
BLOCK = 128
TALL = 256
WINDOW = 64
MARGIN = 16
BOUNDS = 16
MEGA = 1024 * 1024
RATE = 1150000000
F32 = jnp.float32
BF16 = jnp.bfloat16


def dot_nn(left, right):
    return jnp.dot(left, right, preferred_element_type=F32)


def dot_nt(left, right):
    return lax.dot_general(left, right, (((1,), (1,)), ((), ())), preferred_element_type=F32)


def dot_tn(left, right):
    return lax.dot_general(left, right, (((0,), (0,)), ((), ())), preferred_element_type=F32)


def rows_of(index, size, base=0):
    return pl.ds(pl.multiple_of(index * size, size) + base, size)


def line_of(ref):
    return ref[...].astype(F32).reshape(1, ref.shape[0])


def fold_rows(values):
    return jnp.sum(values.reshape(values.shape[0] // 8, 8, values.shape[1]), axis=0)


def one_row(values):
    return jnp.sum(values, axis=0, keepdims=True)


def turn(values):
    return pltpu.roll(values, LOW, 1)


def low_lanes(rows):
    return lax.broadcasted_iota(jnp.int32, (rows, LANES), 1) < LOW


def centre_rows(inputs):
    mean = jnp.mean(inputs, axis=-1, keepdims=True)
    centred = inputs - mean
    spread = jnp.mean(centred * centred, axis=-1, keepdims=True)
    return centred * lax.rsqrt(spread + EPS)


ERF_SCALE = 0.3275911 / math.sqrt(2.0)
ERF_TERMS = tuple(0.5 * term for term in (1.061405429, -1.453152027, 1.421413741, -0.284496736, 0.254829592))


def normal_parts(values):
    bell = jnp.exp(values * values * -0.5)
    size = 1.0 + ERF_SCALE * jnp.abs(values)
    place = pl.reciprocal(size, approx=True)
    place = place * (2.0 - size * place)
    series = ERF_TERMS[0]
    for term in ERF_TERMS[1:]:
        series = series * place + term
    tail = series * place * bell
    return jnp.where(values < 0.0, tail, 1.0 - tail), bell


def gelu_parts(values):
    phi, bell = normal_parts(values)
    return values * phi, phi + values * bell * (1.0 / math.sqrt(2.0 * math.pi))


class Part:
    def __init__(self, shape=None, pairs=None, refs=1, late=False):
        self.shape, self.pairs, self.refs, self.late = shape, pairs, refs, late

    def buffer(self, operand):
        return self.shape or operand.shape

    def copies(self, refs, buffer):
        return self.pairs(refs, buffer) if self.pairs else [(refs[0], buffer)]


def blocks_part():
    def pairs(refs, buffer):
        place = lax.axis_index("tm")
        return [
            (ref, buffer.at[rows_of(lax.bitwise_xor(jnp.int32(apart), place), BLOCK)])
            for apart, ref in enumerate(refs)
        ]

    return Part((HEADS * BLOCK, D), pairs, HEADS)


def rows_part(first, size, late=False):
    return Part((size, D), lambda refs, buffer: [(refs[0].at[pl.ds(first, size)], buffer)], late=late)


class Fetch:
    def __init__(self, pairs, buffer, sems, first):
        self.buffer, self.begun = buffer, False
        self.pending = [
            pltpu.make_async_copy(source, target, sems.at[first + index])
            for index, (source, target) in enumerate(pairs)
        ]

    def begin(self):
        if not self.begun:
            for copy in self.pending:
                copy.start()
        self.begun = True

    def __call__(self):
        self.begin()
        for copy in self.pending:
            copy.wait()
        self.pending = []
        return self.buffer


def begin(*fetches):
    for fetch in fetches:
        fetch.begin()


class Send:
    def __init__(self, buffer, target, sems):
        self.buffer, self.target, self.sems, self.copies = buffer, target, sems, []

    def go(self, *index):
        source, target = (self.buffer.at[index], self.target.at[index]) if index else (self.buffer, self.target)
        copy = pltpu.make_async_copy(source, target, self.sems[len(self.copies)])
        copy.start()
        self.copies.append(copy)

    def finish(self):
        if not self.copies:
            self.go()


SPACES = {"v": pltpu.VMEM, "s": pltpu.SMEM, "k": pl.ANY}


def kernel_call(body, out_shapes, plan, scratch=(), micros=2, megas=58, bounds=False, aliases=None):
    def call(*operands):
        in_specs, buffers, at = [], [], 0
        for item in plan:
            if isinstance(item, Part):
                in_specs += [pl.BlockSpec(memory_space=pl.ANY)] * item.refs
                buffers.append(pltpu.VMEM(item.buffer(operands[at]), operands[at].dtype))
                at += item.refs
            else:
                in_specs.append(pl.BlockSpec(memory_space=SPACES[item]))
                at += 1
        sent = [out for out in out_shapes if len(out) > 2]
        buffers += [pltpu.VMEM(out[3] if len(out) > 3 else out[0], out[1]) for out in sent]
        sem_count = 64
        extra = [pltpu.SMEM((BOUNDS,), jnp.int32)] if bounds else []

        def outer(*refs):
            inputs, rest = refs[: len(in_specs)], refs[len(in_specs) :]
            outputs, rest = rest[: len(out_shapes)], rest[len(out_shapes) :]
            held, rest = list(rest[: len(buffers)]), rest[len(buffers) :]
            sems, rest = rest[0], rest[1:]
            given, at, used = [], 0, 0
            for item in plan:
                if isinstance(item, Part):
                    buffer = held.pop(0)
                    pairs = item.copies(inputs[at : at + item.refs], buffer)
                    given.append(Fetch(pairs, buffer, sems, used))
                    if not item.late:
                        given[-1].begin()
                    used += len(pairs)
                    at += item.refs
                else:
                    given.append(inputs[at])
                    at += 1
            results = []
            for out, ref in zip(out_shapes, outputs):
                if len(out) > 2:
                    target = out[4](ref) if len(out) > 3 else ref
                    results.append(Send(held.pop(0), target, [sems.at[used], sems.at[used + 1]]))
                    used += 2
                else:
                    results.append(ref)
            assert used <= sem_count
            body(*given, *results, *rest)
            for item in given:
                if isinstance(item, Fetch):
                    item()
            sends = [item for item in results if isinstance(item, Send)]
            for item in sends:
                item.finish()
            for item in sends:
                for copy in item.copies:
                    copy.wait()

        return pl.pallas_call(
            outer,
            out_shape=[jax.ShapeDtypeStruct(out[0], out[1]) for out in out_shapes],
            in_specs=in_specs,
            out_specs=[pl.BlockSpec(memory_space=pl.ANY if len(out) > 2 else pltpu.VMEM) for out in out_shapes],
            scratch_shapes=buffers
            + [pltpu.SemaphoreType.DMA((sem_count,))]
            + [pltpu.VMEM(shape, kind) for shape, kind in scratch]
            + extra,
            input_output_aliases=aliases or {},
            compiler_params=pltpu.CompilerParams(vmem_limit_bytes=megas * MEGA),
            cost_estimate=pl.CostEstimate(flops=micros * RATE, bytes_accessed=1 << 20, transcendentals=0),
        )(*operands)

    return call


def fill_bounds(lengths_ref, bounds_s, total):
    bounds_s[0] = jnp.int32(0)
    end = jnp.int32(0)
    for item in range(ITEMS):
        end = end + lengths_ref[0, item]
        bounds_s[item + 1] = end
    for item in range(ITEMS + 1, BOUNDS):
        bounds_s[item] = jnp.int32(total)


def select_kernel(
    up_ref,
    up_bias_ref,
    gain_ref,
    bias_ref,
    conv_bias_ref,
    taps_ref,
    qkv_ref,
    pos_ref,
    content_ref,
    position_ref,
    up_out,
    table_out,
    qkv_out,
    pos_out,
    bias_out,
):
    place = lax.axis_index("tm")
    quarters = lax.axis_size("stream")
    share = HALF // (quarters * lax.axis_size("tm"))
    lane = lax.broadcasted_iota(jnp.int32, (1, 2 * LANES), 1)
    channel = jnp.where(lane < LANES + LOW, lane, lane - LOW)
    group = jnp.zeros_like(channel)
    for quarter in range(1, quarters):
        group = group + (channel >= quarter * share).astype(jnp.int32)
    source = group * (HALF // quarters) + share * place + channel - group * share
    chosen = (lax.broadcasted_iota(jnp.int32, (HALF, 2 * LANES), 0) == source).astype(F32).astype(BF16)
    gate = dot_nn(up_ref[:, :HALF], chosen)
    conv = dot_nn(up_ref[:, HALF:], chosen)
    up_out[:, :LANES] = gate[:, :LANES].astype(BF16)
    up_out[:, LANES : 2 * LANES] = jnp.where(low_lanes(D), gate[:, LANES:], conv[:, LANES:]).astype(BF16)
    up_out[:, 2 * LANES :] = conv[:, :LANES].astype(BF16)
    up_bias = line_of(up_bias_ref)
    lines = jnp.concatenate(
        [
            up_bias[:, :HALF],
            up_bias[:, HALF:],
            line_of(gain_ref),
            line_of(bias_ref),
            line_of(conv_bias_ref),
            jnp.zeros((3, HALF), F32),
        ],
        axis=0,
    )
    lines = dot_nn(lines.astype(BF16), chosen)
    taps = dot_nn(taps_ref[...], chosen)
    for part in range(2):
        lanes = slice(part * LANES, (part + 1) * LANES)
        table_out[part, :8] = lines[:, lanes]
        table_out[part, 8 : 8 + KERNEL] = taps[:, lanes]
        table_out[part, 8 + KERNEL :] = jnp.zeros((1, LANES), F32)

    odd = lax.rem(place, 2) == 1

    def head_lanes(ref, base):
        at = pl.ds(pl.multiple_of(lax.div(place, 2) * LANES + base, LANES), LANES)
        values = ref[:, at].astype(F32)
        values = jnp.where(odd, turn(values), values)
        return jnp.where(low_lanes(values.shape[0]), values, 0.0)

    for part in range(3):
        qkv_out[:, part * LANES : (part + 1) * LANES] = head_lanes(qkv_ref, part * D).astype(BF16)
    pos_out[...] = head_lanes(pos_ref, 0).astype(BF16)
    bias_out[...] = jnp.zeros((8, LANES), F32)
    for line, ref in enumerate((content_ref, position_ref)):
        values = line_of(ref)
        picked = values[:, :LANES]
        for tile in range(1, D // LANES):
            picked = jnp.where(
                lax.div(place, 2) == tile, values[:, tile * LANES : (tile + 1) * LANES], picked
            )
        picked = jnp.where(odd, turn(picked), picked)
        bias_out[line : line + 1] = jnp.where(low_lanes(1), picked, 0.0)


def angle_rows(coarse_ref, fine_ref, block, rows):
    half = D // 2
    base = coarse_ref[pl.ds(block, 1)]
    base_sine, base_cosine = base[:, :half], base[:, half:]
    sine, cosine = fine_ref[rows, :half], fine_ref[rows, half:]
    return base_sine * cosine + base_cosine * sine, base_cosine * cosine - base_sine * sine


def item_codes(bounds_s, index):
    code = jnp.zeros_like(index)
    for item in range(1, ITEMS + 1):
        code = code + (index >= bounds_s[item]).astype(jnp.int32)
    return jnp.where(code < ITEMS, code, ITEMS + index)


def attend_kernel(
    lengths_ref,
    x_ref,
    attn_gain_ref,
    attn_bias_ref,
    mlp_gain_ref,
    mlp_bias_ref,
    qkv_ref,
    pos_ref,
    bias_ref,
    coarse_ref,
    fine_ref,
    up_ref,
    up_bias_ref,
    n_attn_out,
    n_mlp_out,
    hat_out,
    q_position_out,
    query_out,
    key_out,
    value_out,
    prob_out,
    attn_out,
    share_out,
    stats_out,
    pre_s,
    bounds_s,
):
    frames = n_attn_out.buffer.shape[0]
    half = D // 2
    fill_bounds(lengths_ref, bounds_s, frames)
    attn_gain, attn_bias = line_of(attn_gain_ref), line_of(attn_bias_ref)
    mlp_gain, mlp_bias = line_of(mlp_gain_ref), line_of(mlp_bias_ref)
    content, position = bias_ref[0:1], bias_ref[1:2]
    x_ref = x_ref()
    begin(up_ref)

    @pl.loop(0, frames // TALL, unroll=2)
    def _(block):
        rows = rows_of(block, TALL)
        for part in range(TALL // 32):
            at = rows_of(block, TALL, part * 32)
            at = pl.ds(pl.multiple_of(block * TALL + part * 32, 32), 32)
            hat = centre_rows(x_ref[at].astype(F32))
            hat_out.buffer[at] = hat.astype(BF16)
            n_attn_out.buffer[at] = (hat * attn_gain + attn_bias).astype(BF16)
            n_mlp_out.buffer[at] = (hat * mlp_gain + mlp_bias).astype(BF16)
        parts = dot_nn(n_attn_out.buffer[rows], qkv_ref[...])
        query = parts[:, :LANES]
        query_out.buffer[rows, :LANES] = ((query + content).astype(BF16).astype(F32) * 0.125).astype(BF16)
        q_position = (query + position).astype(BF16)
        q_position_out.buffer[rows] = q_position
        key_out.buffer[rows, :LANES] = parts[:, LANES : 2 * LANES].astype(BF16)
        value_out.buffer[rows] = parts[:, 2 * LANES :].astype(BF16)
        projected = dot_nt(q_position, pos_ref[...])
        for part in range(TALL // 32):
            at = pl.ds(pl.multiple_of(block * TALL + part * 32, 32), 32)
            inner = part * 32 % BLOCK
            sine, cosine = angle_rows(
                coarse_ref, fine_ref, block * (TALL // BLOCK) + part * 32 // BLOCK, slice(inner, inner + 32)
            )
            first = projected[part * 32 : part * 32 + 32, :half]
            second = projected[part * 32 : part * 32 + 32, half:]
            query_out.buffer[at, LANES : LANES + half] = ((first * sine + second * cosine) * 0.125).astype(BF16)
            query_out.buffer[at, LANES + half :] = ((second * sine - first * cosine) * 0.125).astype(BF16)
            key_out.buffer[at, LANES : LANES + half] = cosine.astype(BF16)
            key_out.buffer[at, LANES + half :] = sine.astype(BF16)

    for out in (n_attn_out, n_mlp_out, hat_out, q_position_out, query_out, key_out, value_out):
        out.go()
    up_ref = up_ref()
    up_bias = line_of(up_bias_ref)[:, HALF:]
    lane = lax.broadcasted_iota(jnp.int32, (16, LANES), 1)

    @pl.loop(0, frames // BLOCK)
    def _(block):
        pre_s[...] = dot_nn(n_mlp_out.buffer[rows_of(block, BLOCK)], up_ref[...])
        for part in range(BLOCK // 16):
            pre = pre_s[part * 16 : part * 16 + 16] + up_bias
            hidden = pre * (0.5 + 0.5 * lax.erf(pre * math.sqrt(0.5)))
            mean = jnp.mean(hidden, axis=-1, keepdims=True)
            centred = hidden - mean
            rate = lax.rsqrt(jnp.mean(centred * centred, axis=-1, keepdims=True) + EPS)
            at = pl.ds(pl.multiple_of(block * BLOCK + part * 16, 16), 16)
            stats_out.buffer[at] = jnp.where(lane == 0, mean, rate)

    stats_out.go()
    key_code = item_codes(bounds_s, lax.broadcasted_iota(jnp.int32, (1, frames), 1))

    @pl.loop(0, frames // TALL, unroll=2)
    def _(block):
        rows = rows_of(block, TALL)
        raw = dot_nt(query_out.buffer[rows], key_out.buffer[...])
        for part in range(TALL // 32):
            start = block * TALL + part * 32
            at = pl.ds(pl.multiple_of(start, 32), 32)
            index = start + lax.broadcasted_iota(jnp.int32, (32, 1), 0)
            scaled = jnp.where(
                item_codes(bounds_s, index) == key_code, raw[part * 32 : part * 32 + 32], MASKED
            )
            weight = jnp.exp(scaled - jnp.max(scaled, axis=1, keepdims=True))
            prob_out.buffer[at] = weight.astype(BF16)
            share_out.buffer[at] = jnp.broadcast_to(1.0 / jnp.sum(weight, axis=1, keepdims=True), (32, LANES))
        attn_out.buffer[rows] = (
            dot_nn(prob_out.buffer[rows], value_out.buffer[...]) * share_out.buffer[rows]
        )


def fill_margins(wide_s, frames):
    edge = jnp.zeros((MARGIN, LANES), F32)
    wide_s[:MARGIN] = edge
    wide_s[MARGIN + frames : 2 * MARGIN + frames] = edge
    base = frames + 3 * MARGIN
    after = base + frames // 2
    low = low_lanes(MARGIN)
    wide_s[base - MARGIN : base] = jnp.where(low, 0.0, turn(wide_s[after - MARGIN : after]))
    wide_s[after : after + MARGIN] = jnp.where(low, turn(wide_s[base : base + MARGIN]), 0.0)


def item_span(bounds_s, frame):
    begin, end = bounds_s[0], bounds_s[BOUNDS - 1]
    for item in range(1, ITEMS + 1):
        edge = bounds_s[item]
        begin = jnp.where(frame >= edge, edge, begin)
    for item in range(ITEMS, 0, -1):
        edge = bounds_s[item]
        end = jnp.where(frame < edge, edge, end)
    return begin, end


def is_whole(bounds_s, start):
    begin, end = item_span(bounds_s, start)
    reach = KERNEL // 2
    low = (begin == 0) | (begin <= start - reach)
    high = (end == bounds_s[BOUNDS - 1]) | (end >= start + WINDOW + reach)
    return low & high & (end >= start + WINDOW)


def tap_limits(bounds_s, start):
    frame = start + lax.broadcasted_iota(jnp.int32, (WINDOW, LANES), 0)
    begin, end = item_span(bounds_s, frame)
    return begin - frame, end - frame


def grouped(values):
    return values.reshape(WINDOW // 8, 8, LANES)


def triple_places(step, frames):
    half = frames // 2
    return (
        pl.multiple_of(step * WINDOW, 2 * MARGIN),
        pl.multiple_of(step * WINDOW + half, 2 * MARGIN),
        pl.multiple_of(step * WINDOW + frames + 2 * MARGIN, 2 * MARGIN),
    )


def over_windows(bounds_s, frames, body):
    half = frames // 2

    @pl.loop(0, half // WINDOW)
    def _(step):
        start = step * WINDOW
        whole = is_whole(bounds_s, start) & is_whole(bounds_s, start + half)

        @pl.when(whole)
        def _():
            body(step, None)

        @pl.when(jnp.logical_not(whole))
        def _():
            first, second = tap_limits(bounds_s, start), tap_limits(bounds_s, start + half)
            low = low_lanes(WINDOW)
            rest = [jnp.where(low, one, other) for one, other in zip(first, second)]
            body(step, (first, second, rest))


def tap_view(window_ref, tap, limits):
    view = window_ref[tap + 1 : tap + 1 + WINDOW]
    if limits is not None:
        shift = tap - KERNEL // 2
        view = jnp.where((limits[0] <= shift) & (limits[1] > shift), view, 0.0)
    return grouped(view)


def mlp_first_kernel(
    lengths_ref,
    n_ref,
    up_ref,
    table_ref,
    stats_ref,
    cot_ref,
    merge_ref,
    down_ref,
    attn_ref,
    mixed_out,
    gate_pre_out,
    grad_out,
    rate_out,
    hat_out,
    early_out,
    vectors_out,
    lines_out,
    hat_s,
    slope_s,
    gate_s,
    hidden_s,
    gate_slope_s,
    conv_s,
    grad_s,
    out_s,
    back_s,
    branch_s,
    mix_s,
    taps_s,
    turn_s,
    tap_sum_s,
    columns_s,
    forward_s,
    backward_s,
    bounds_s,
):
    frames = mix_s.shape[0]
    half = frames // 2
    blocks = frames // BLOCK
    quarters, early_rows, _ = early_out.buffer.shape
    share = early_rows // 8
    channels = quarters * share
    fill_bounds(lengths_ref, bounds_s, frames)
    for part in range(2):
        for tap in range(KERNEL):
            line = jnp.broadcast_to(table_ref[part, 8 + tap : 9 + tap], (8, LANES))
            taps_s[part, tap] = line
            turn_s[part, KERNEL - 1 - tap] = line
    tap_sum_s[...] = jnp.zeros(tap_sum_s.shape, F32)
    main, rest = table_ref[0, :8], table_ref[1, :8]
    mixed_bias = jnp.where(low_lanes(1), rest[0:1], rest[1:2])
    low = low_lanes(64)
    gate_pre_ref = gate_pre_out.buffer
    n_ref = n_ref()
    stats_ref = stats_ref()
    begin(cot_ref, merge_ref, down_ref, attn_ref)

    def stat_rows(rows):
        stats = stats_ref[rows]
        return stats[:, 0:1], stats[:, 1:2]

    def chunk(start, base=0):
        return pl.ds(pl.multiple_of(start, 64) + base, 64)

    def conv_part(hidden, mean, rate, lines, rows, to_rows):
        hat = (hidden - mean) * rate
        hat_s[rows] = hat
        hat_out.buffer[rows] = hat.astype(BF16)
        conv_s[to_rows] = (hat * lines[2:3] + lines[3:4]).astype(BF16).astype(F32)

    @pl.loop(0, half // TALL)
    def _(block):
        pre = [dot_nn(n_ref[rows_of(block, TALL, base)], up_ref[...]) for base in (0, half)]
        for part in range(TALL // 64):
            inner = slice(part * 64, part * 64 + 64)
            start = block * TALL + part * 64
            mixed = []
            for values, base in zip(pre, (0, half)):
                rows = chunk(start, base)
                gate, gate_slope = gelu_parts(values[inner, :LANES] + main[0:1])
                hidden_s[rows] = gate
                gate_slope_s[rows] = gate_slope
                hidden, slope = gelu_parts(values[inner, 2 * LANES :] + main[1:2])
                mean, rate = stat_rows(rows)
                slope_s[rows] = slope * rate
                conv_part(hidden, mean, rate, main, rows, chunk(start, base + MARGIN))
                mixed.append((*gelu_parts(values[inner, LANES : 2 * LANES] + mixed_bias), mean, rate))
            (low_hidden, low_slope, low_mean, low_rate), (high_hidden, high_slope, high_mean, high_rate) = mixed
            rows = chunk(start, frames)
            hidden_s[rows] = jnp.where(low, low_hidden, turn(high_hidden))
            gate_slope_s[rows] = jnp.where(low, low_slope, turn(high_slope))
            rate = jnp.where(low, low_rate, high_rate)
            slope_s[rows] = jnp.where(low, turn(low_slope), high_slope) * rate
            conv_part(
                jnp.where(low, turn(low_hidden), high_hidden),
                jnp.where(low, low_mean, high_mean),
                rate,
                rest,
                rows,
                chunk(start, frames + 3 * MARGIN),
            )

    hat_out.go()
    fill_margins(conv_s, frames)
    tall = WINDOW + 2 * MARGIN
    outs = (0, half, frames)

    def convolve(step, limits):
        for index, base in enumerate(triple_places(step, frames)):
            forward_s[index] = conv_s[pl.ds(base, tall)]
        for index in range(3):
            own = None if limits is None else limits[index]
            total = jnp.zeros((WINDOW // 8, 8, LANES), F32)
            for tap in range(KERNEL):
                total = total + tap_view(forward_s.at[index], tap, own) * taps_s[index // 2, tap][None]
            lines = rest if index == 2 else main
            out_s[rows_of(step, WINDOW, outs[index])] = total.reshape(WINDOW, LANES) + lines[4:5]

    over_windows(bounds_s, frames, convolve)
    cot_ref = cot_ref()
    merge_ref = merge_ref()
    down_ref = down_ref()
    attn_ref = attn_ref()
    down_ref[channels:] = jnp.zeros((2 * LANES - channels, D), BF16)
    zero = jnp.zeros((8, LANES), F32)

    def branch_part(grad_gated, rows, to_rows, sums):
        up_sum, conv_sum = sums
        gate, conv = hidden_s[rows], out_s[rows]
        gate_pre = (grad_gated * conv * gate_slope_s[rows]).astype(BF16)
        gate_pre_ref[rows] = gate_pre
        grad_conv = (grad_gated * gate).astype(BF16).astype(F32)
        grad_s[to_rows] = grad_conv
        gate_pre = gate_pre.astype(F32)
        return gate * conv, gate_pre, (up_sum + fold_rows(gate_pre), conv_sum + fold_rows(grad_conv))

    def branch_step(block, sums):
        main_sums, rest_sums = sums
        grads = []
        for base in (0, half):
            rows = rows_of(block, TALL, base)
            branch = dot_nt(cot_ref[rows], merge_ref[...]).astype(BF16)
            branch_s[rows] = branch
            grads.append(dot_nt(branch, down_ref[...]))
        for part in range(TALL // 64):
            inner = slice(part * 64, part * 64 + 64)
            start = block * TALL + part * 64
            for values, base in zip(grads, (0, half)):
                rows = chunk(start, base)
                gated, gate_pre, main_sums = branch_part(
                    values[inner, :LANES], rows, chunk(start, base + MARGIN), main_sums
                )
                mix_s[rows, :LANES] = gated.astype(BF16)
                gate_s[rows, :LANES] = gate_pre.astype(BF16)
            grad = jnp.where(low, grads[0][inner, LANES:], turn(grads[1][inner, LANES:]))
            gated, gate_pre, rest_sums = branch_part(
                grad, chunk(start, frames), chunk(start, frames + 3 * MARGIN), rest_sums
            )
            low_rows, high_rows = chunk(start), chunk(start, half)
            gate_s[low_rows, LANES:] = gate_pre.astype(BF16)
            gate_s[high_rows, LANES:] = turn(gate_pre).astype(BF16)
            mix_s[low_rows, LANES:] = jnp.where(low, gated, turn(attn_ref[low_rows])).astype(BF16)
            mix_s[high_rows, LANES:] = jnp.where(low, turn(gated), turn(attn_ref[high_rows])).astype(BF16)
        return main_sums, rest_sums

    (main_up, main_conv), (rest_up, rest_conv) = lax.fori_loop(
        0, half // TALL, branch_step, ((zero, zero), (zero, zero))
    )
    gate_pre_out.go()
    fill_margins(grad_s, frames)
    ones = jnp.ones((16, frames), BF16)
    lines_out[0:1] = dot_nn(ones, branch_s[...])[0:1]
    lines_out[1:2] = dot_nn(ones, cot_ref[...])[0:1]
    lines_out[2:8] = jnp.zeros((6, D), F32)
    grad_down = dot_tn(mix_s[...], branch_s[...])
    grad_gate = dot_tn(gate_s[...], n_ref[...])
    for quarter in range(quarters):
        for tile in range(4):
            early_out.buffer[quarter, tile * share : (tile + 1) * share] = grad_down[
                quarter * share : (quarter + 1) * share, tile * LANES : (tile + 1) * LANES
            ].astype(BF16)
        early_out.buffer[quarter, 4 * share :] = grad_gate[
            :channels, quarter * LANES : (quarter + 1) * LANES
        ].astype(BF16)

    early_out.go()
    for block in range(blocks):
        mixed_out.buffer[block, :BLOCK] = mix_s[block * BLOCK : (block + 1) * BLOCK]
    mixed_out.go(slice(None), pl.ds(0, BLOCK))

    def differentiate(step, limits):
        for index, base in enumerate(triple_places(step, frames)):
            forward_s[index] = conv_s[pl.ds(base, tall)]
            backward_s[index] = grad_s[pl.ds(base, tall)]
        for index in range(3):
            own = None if limits is None else limits[index]
            total = jnp.zeros((WINDOW // 8, 8, LANES), F32)
            centre = grouped(backward_s[index, MARGIN : MARGIN + WINDOW])
            for tap in range(KERNEL):
                total = total + tap_view(backward_s.at[index], tap, own) * turn_s[index // 2, tap][None]
                tap_sum_s[index // 2, tap] += jnp.sum(tap_view(forward_s.at[index], tap, own) * centre, axis=0)
            back_s[rows_of(step, WINDOW, outs[index])] = total.reshape(WINDOW, LANES)

    over_windows(bounds_s, frames, differentiate)
    lane = lax.broadcasted_iota(jnp.int32, (64, LANES), 1)

    def norm_part(rows, lines, sums):
        gain_sum, bias_sum = sums
        back, hat, slope = back_s[rows], hat_s[rows], slope_s[rows]
        grad = back * lines[2:3]
        grad_out.buffer[rows] = (grad * slope).astype(BF16)
        rate_out.buffer[rows] = slope.astype(BF16)
        along = back * hat
        return grad, along * lines[2:3], (gain_sum + fold_rows(along), bias_sum + fold_rows(back))

    def norm_step(block, sums):
        main_sums, rest_sums = sums
        for part in range(TALL // 64):
            start = block * TALL + part * 64
            pairs = []
            for base in (0, half):
                plain, along, main_sums = norm_part(chunk(start, base), main, main_sums)
                pairs.append([plain, along])
            plain, along, rest_sums = norm_part(chunk(start, frames), rest, rest_sums)
            for item, values in enumerate((plain, along)):
                pairs[0][item] = pairs[0][item] + jnp.where(low, values, 0.0)
                pairs[1][item] = pairs[1][item] + jnp.where(low, 0.0, values)
            for (plain, along), base in zip(pairs, (0, half)):
                columns_s[chunk(start, base)] = jnp.where(
                    lane == 0,
                    jnp.sum(plain, axis=-1, keepdims=True),
                    jnp.where(lane == 1, jnp.sum(along, axis=-1, keepdims=True), 0.0),
                )
        return main_sums, rest_sums

    (main_gain, main_bias), (rest_gain, rest_bias) = lax.fori_loop(
        0, half // TALL, norm_step, ((zero, zero), (zero, zero))
    )
    grad_out.go()
    rate_out.go()
    totals = jnp.concatenate(
        [jnp.transpose(columns_s[block * BLOCK : (block + 1) * BLOCK])[:2] for block in range(blocks)], axis=0
    )
    high = totals.astype(BF16)
    low_part = (totals - high.astype(F32)).astype(BF16)
    for block in range(blocks):
        mixed_out.buffer[block, BLOCK:, :LANES] = high
        mixed_out.buffer[block, BLOCK:, LANES:] = low_part
    mixed_out.go(slice(None), pl.ds(BLOCK, 2 * blocks))

    def vectors(part, lines):
        taps = jnp.sum(tap_sum_s[part], axis=1)[:KERNEL]
        stacked = jnp.concatenate([taps] + [one_row(line) for line in lines], axis=0)
        if part:
            stacked = stacked + turn(stacked)
        return jnp.transpose(
            jnp.concatenate([stacked, jnp.zeros((LANES - stacked.shape[0], LANES), F32)], axis=0)
        )

    vectors_out[:LANES] = vectors(0, (main_conv, main_gain, main_bias, main_up))
    vectors_out[LANES:] = vectors(1, (rest_conv, rest_gain, rest_bias, rest_up))[: channels - LANES]


def attend_back_kernel(
    cot_ref,
    merge_ref,
    head_ref,
    share_ref,
    value_ref,
    attn_ref,
    prob_ref,
    key_ref,
    coarse_ref,
    fine_ref,
    pos_ref,
    query_ref,
    n_ref,
    q_position_ref,
    qkv_ref,
    hat_ref,
    gain_ref,
    early_ref,
    branch_out,
    total_out,
    pack_out,
    lines_out,
    grad_s,
    raw_s,
    projected_s,
    parts_s,
    grads_s,
):
    place = lax.axis_index("tm")
    frames = raw_s.shape[0]
    blocks = frames // BLOCK
    half = D // 2
    zero = jnp.zeros((8, LANES), F32)
    cot_ref, merge_ref, head_ref, share_ref = cot_ref(), merge_ref(), head_ref(), share_ref()
    head_ref[HEAD:] = jnp.zeros((LANES - HEAD, D), BF16)
    begin(value_ref, attn_ref, prob_ref, key_ref, pos_ref)

    @pl.loop(0, frames // TALL, unroll=2)
    def _(block):
        rows = rows_of(block, TALL)
        branch = dot_nt(cot_ref[rows], merge_ref[...]).astype(BF16)
        branch_out.buffer[rows] = branch
        grad_s[rows] = (dot_nt(branch, head_ref[...]) * share_ref[rows]).astype(BF16)

    branch_out.go()
    value_ref, attn_ref, prob_ref = value_ref(), attn_ref(), prob_ref()
    key_ref, pos_ref = key_ref(), pos_ref()
    begin(query_ref, n_ref, q_position_ref, qkv_ref, hat_ref, early_ref)

    def score_step(block, sums):
        content_sum, position_sum = sums
        rows = rows_of(block, TALL)
        grad = grad_s[rows]
        score = dot_nt(grad, value_ref[...])
        for part in range(TALL // 32):
            at = pl.ds(pl.multiple_of(block * TALL + part * 32, 32), 32)
            inner = slice(part * 32, part * 32 + 32)
            delta = jnp.sum(grad[inner].astype(F32) * attn_ref[at], axis=1, keepdims=True)
            raw_s[at] = (prob_ref[at].astype(F32) * (score[inner] - delta)).astype(BF16)
        query = dot_nn(raw_s[rows], key_ref[...]) * 0.125
        for part in range(TALL // 32):
            at = pl.ds(pl.multiple_of(block * TALL + part * 32, 32), 32)
            inner = part * 32 % BLOCK
            sine, cosine = angle_rows(
                coarse_ref, fine_ref, block * (TALL // BLOCK) + part * 32 // BLOCK, slice(inner, inner + 32)
            )
            inner = slice(part * 32, part * 32 + 32)
            first, second = query[inner, LANES : LANES + half], query[inner, LANES + half :]
            projected_s[at, :half] = (first * sine - second * cosine).astype(BF16)
            projected_s[at, half:] = (first * cosine + second * sine).astype(BF16)
        position = dot_nn(projected_s[rows], pos_ref[...])
        content = query[:, :LANES]
        parts_s[rows, :LANES] = (content + position).astype(BF16)
        return content_sum + fold_rows(content), position_sum + fold_rows(position)

    content_sum, position_sum = lax.fori_loop(0, frames // TALL, score_step, (zero, zero), unroll=2)
    query_ref, n_ref, q_position_ref = query_ref(), n_ref(), q_position_ref()
    qkv_ref, hat_ref = qkv_ref(), hat_ref()
    grad_key = dot_tn(query_ref[...], raw_s[...])
    grad_value = dot_tn(grad_s[...], prob_ref[...])
    for block in range(blocks):
        at = slice(block * BLOCK, (block + 1) * BLOCK)
        parts_s[at, LANES : 2 * LANES] = jnp.transpose(grad_key[:, at]).astype(BF16)
        parts_s[at, 2 * LANES :] = jnp.transpose(grad_value[:, at]).astype(BF16)
    grads_s[:HEAD] = dot_tn(parts_s[:, :LANES], n_ref[...])[:HEAD]
    grads_s[HEAD : 2 * HEAD] = dot_nn(grad_key.astype(BF16), n_ref[...])[:HEAD]
    grads_s[2 * HEAD : 3 * HEAD] = dot_nn(grad_value.astype(BF16), n_ref[...])[:HEAD]
    grads_s[3 * HEAD :] = dot_tn(q_position_ref[...], projected_s[...])[:HEAD]
    for quarter in range(pack_out.buffer.shape[0]):
        pack_out.buffer[quarter, : 4 * HEAD] = grads_s[:, quarter * LANES : (quarter + 1) * LANES].astype(BF16)
    pack_out.buffer[:, 4 * HEAD :] = early_ref()[...]
    pack_out.go()
    gain = line_of(gain_ref)
    wide_zero = jnp.zeros((8, D), F32)

    def norm_step(block, sums):
        gain_sum, bias_sum = sums
        grad = dot_nt(parts_s[rows_of(block, TALL)], qkv_ref[...])
        for part in range(TALL // 32):
            at = pl.ds(pl.multiple_of(block * TALL + part * 32, 32), 32)
            own = grad[part * 32 : part * 32 + 32]
            total_out.buffer[at] = (own * gain).astype(BF16)
            gain_sum = gain_sum + fold_rows(own * hat_ref[at].astype(F32))
            bias_sum = bias_sum + fold_rows(own)
        return gain_sum, bias_sum

    gain_sum, bias_sum = lax.fori_loop(0, frames // TALL, norm_step, (wide_zero, wide_zero), unroll=2)
    lane = lax.broadcasted_iota(jnp.int32, (1, LANES), 1)

    def own_lanes(sums):
        line = one_row(sums)
        line = line + turn(line)
        tiles = [
            jnp.where(lax.div(tile * LANES + lane, HEAD) == place, line, 0.0) for tile in range(D // LANES)
        ]
        return jnp.concatenate(tiles, axis=1)

    lines_out[...] = jnp.concatenate(
        [
            one_row(gain_sum),
            one_row(bias_sum),
            own_lanes(content_sum),
            own_lanes(position_sum),
            jnp.zeros((4, D), F32),
        ],
        axis=0,
    )


def mlp_second_kernel(
    mixed_ref,
    gate_pre_ref,
    grad_ref,
    rate_ref,
    hat_ref,
    up_ref,
    norm_hat_ref,
    gain_ref,
    other_ref,
    n_ref,
    vectors_ref,
    first_lines_ref,
    head_lines_ref,
    same_out,
    apart_out,
    pack_0,
    pack_1,
    pack_2,
    pack_3,
    pre_s,
    columns_s,
    grad_up_s,
    lines_s,
    up_columns_s,
):
    packs = (pack_0, pack_1, pack_2, pack_3)
    stream = lax.axis_index("stream")
    place = lax.axis_index("tm")
    frames = pre_s.shape[0]
    half = frames // 2
    blocks = frames // BLOCK
    quarters = len(packs)
    channels = vectors_ref.shape[0]
    share = channels // quarters
    totals = jnp.zeros((2 * blocks, LANES), F32)
    mixed_ref = mixed_ref()
    for source in range(mixed_ref.shape[0]):
        both = mixed_ref[source].astype(F32)
        totals = totals + (both[:, :LANES] + both[:, LANES:])
    totals = totals * (1.0 / HALF)
    columns = jnp.transpose(jnp.concatenate([totals, jnp.zeros((LANES - 2 * blocks, LANES), F32)], axis=0))
    lane = lax.broadcasted_iota(jnp.int32, (BLOCK, LANES), 1)
    for block in range(blocks):
        columns_s[block * BLOCK : (block + 1) * BLOCK] = jnp.where(
            lane == 0, columns[:, 2 * block : 2 * block + 1], columns[:, 2 * block + 1 : 2 * block + 2]
        )
    gate_pre_ref, grad_ref, rate_ref, hat_ref = gate_pre_ref(), grad_ref(), rate_ref(), hat_ref()
    begin(n_ref, up_ref, norm_hat_ref, other_ref)
    low = low_lanes(64)
    gain = line_of(gain_ref)

    def chunk(start, base=0):
        return pl.ds(pl.multiple_of(start, 64) + base, 64)

    def pre_part(rows, table, up_sum):
        plain, along = table
        hat, rate = hat_ref[rows].astype(F32), rate_ref[rows].astype(F32)
        pre = (grad_ref[rows].astype(F32) - rate * (plain + hat * along)).astype(BF16).astype(F32)
        return pre, up_sum + fold_rows(pre)

    def pre_step(block, sums):
        main_up, rest_up = sums
        for part in range(TALL // 64):
            start = block * TALL + part * 64
            tables = []
            for base in (0, half):
                rows = chunk(start, base)
                values = columns_s[rows]
                table = [values[:, item : item + 1] for item in range(2)]
                tables.append(table)
                pre, main_up = pre_part(rows, table, main_up)
                pre_s[rows, :LANES] = gate_pre_ref[rows]
                pre_s[rows, 2 * LANES :] = pre.astype(BF16)
            rows = chunk(start, frames)
            table = [jnp.where(low, one, other) for one, other in zip(*tables)]
            pre, rest_up = pre_part(rows, table, rest_up)
            gate_pre = gate_pre_ref[rows].astype(F32)
            pre_s[chunk(start), LANES : 2 * LANES] = jnp.where(low, gate_pre, turn(pre)).astype(BF16)
            pre_s[chunk(start, half), LANES : 2 * LANES] = jnp.where(low, turn(gate_pre), pre).astype(BF16)
        return main_up, rest_up

    zero = jnp.zeros((8, LANES), F32)
    main_up, rest_up = lax.fori_loop(0, half // TALL, pre_step, (zero, zero))
    n_ref, up_ref, norm_hat_ref, other_ref = n_ref(), up_ref(), norm_hat_ref(), other_ref()
    grad_up_s[...] = dot_tn(pre_s[:, LANES:], n_ref[...])
    wide_zero = jnp.zeros((8, D), F32)

    def norm_step(block, sums):
        gain_sum, bias_sum = sums
        rows = rows_of(block, BLOCK)
        grad = dot_nt(pre_s[rows], up_ref[...])
        total = (grad * gain + other_ref[rows].astype(F32)).astype(BF16)
        apart = lax.bitwise_xor(block, place)
        slot = lax.div(apart, 2)

        @pl.when(lax.rem(apart, 2) == 0)
        def _():
            same_out.buffer[slot] = total

        @pl.when(lax.rem(apart, 2) == 1)
        def _():
            apart_out.buffer[slot] = total

        return gain_sum + fold_rows(grad * norm_hat_ref[rows].astype(F32)), bias_sum + fold_rows(grad)

    gain_sum, bias_sum = lax.fori_loop(0, blocks, norm_step, (wide_zero, wide_zero), unroll=2)
    apart_out.go()
    same_out.go()
    rest_line = one_row(rest_up)
    up_columns_s[:LANES] = jnp.transpose(jnp.broadcast_to(one_row(main_up), (LANES, LANES)))
    up_columns_s[LANES:] = jnp.transpose(jnp.broadcast_to(rest_line + turn(rest_line), (LANES, LANES)))[:LOW]
    first_device = (place == 0).astype(F32)
    lines_s[...] = jnp.concatenate(
        [
            head_lines_ref[0:2],
            one_row(gain_sum),
            one_row(bias_sum),
            head_lines_ref[2:4],
            first_lines_ref[0:2] * first_device,
            jnp.zeros((8, D), F32),
        ],
        axis=0,
    )
    gate_at = KERNEL + 3
    lane = lax.broadcasted_iota(jnp.int32, (share, LANES), 1)
    for apart, pack_out in enumerate(packs):
        quarter = lax.bitwise_xor(stream, jnp.int32(apart))
        lanes = pl.ds(pl.multiple_of(quarter * LANES, LANES), LANES)
        pack_out[:LANES] = grad_up_s[LANES:, lanes].astype(BF16)
        pack_out[LANES:channels] = grad_up_s[LOW:LANES, lanes].astype(BF16)
        table = vectors_ref[pl.ds(pl.multiple_of(quarter * share, 8), share)]
        for other in range(2):
            at = pl.ds(pl.multiple_of((2 * lax.rem(quarter, 2) + other) * share, 8), share)
            column = jnp.where(
                quarter < quarters // 2, vectors_ref[at][:, gate_at : gate_at + 1], up_columns_s[at][:, 0:1]
            )
            table = jnp.where(lane == gate_at + other, column, table)
        pack_out[channels : channels + share] = table.astype(BF16)
        pack_out[channels + share :] = lines_s[:, lanes].astype(BF16)


def output_kernel(
    x_ref, mixed_ref, head_ref, down_ref, down_bias_ref, merge_ref, merge_bias_ref, out_ref, joined_out
):
    sources = mixed_ref.shape[0]
    rows = x_ref.shape[0]
    channels = HALF // sources
    share = channels // 4
    attn_parts = []
    branch_attn = jnp.zeros((rows, D), F32)
    branch_mlp = jnp.zeros((rows, D), F32)
    for source in range(sources):
        attn = turn(mixed_ref[source, :rows, LANES:].astype(F32))[:, :HEAD].astype(BF16)
        attn_parts.append(attn)
        branch_attn = branch_attn + dot_nn(attn, head_ref[source * HEAD : (source + 1) * HEAD])
        down = jnp.concatenate(
            [down_ref[(part * sources + source) * share : (part * sources + source + 1) * share] for part in range(4)],
            axis=0,
        )
        branch_mlp = branch_mlp + dot_nn(mixed_ref[source, :rows, :channels], down)
    joined = jnp.concatenate(
        [branch_attn.astype(BF16), (branch_mlp + line_of(down_bias_ref)).astype(BF16)], axis=1
    )
    result = x_ref[...].astype(F32) + dot_nn(joined, merge_ref[...]) + line_of(merge_bias_ref)
    out_ref[...] = result.astype(BF16)
    turned = jnp.transpose(joined.astype(F32))
    heads = jnp.transpose(jnp.concatenate(attn_parts, axis=1).astype(F32))
    merge_share = turned.shape[0] // (4 * sources)
    head_share = heads.shape[0] // (4 * sources)
    used = 4 * (merge_share + head_share)
    for target in range(sources):
        for part in range(4):
            at = (part * sources + target) * merge_share
            joined_out[target, part * merge_share : (part + 1) * merge_share] = turned[
                at : at + merge_share
            ].astype(BF16)
            at = (part * sources + target) * head_share
            to = 4 * merge_share + part * head_share
            joined_out[target, to : to + head_share] = heads[at : at + head_share].astype(BF16)
        joined_out[target, used:] = jnp.zeros((joined_out.shape[1] - used, rows), BF16)


def merge_kernel(joined_ref, cot_ref, branch_ref, pack_0, pack_1, pack_2, pack_3, merge_s, head_s):
    stream = lax.axis_index("stream")
    sources, _, rows = joined_ref.shape
    merge_rows = 2 * D // sources
    head_rows = D // sources
    grad_merge = jnp.zeros((merge_rows, D), F32)
    grad_head = jnp.zeros((head_rows, D), F32)
    for source in range(sources):
        at = slice(source * rows, (source + 1) * rows)
        grad_merge = grad_merge + dot_nn(joined_ref[source, :merge_rows], cot_ref[at])
        grad_head = grad_head + dot_nn(joined_ref[source, merge_rows : merge_rows + head_rows], branch_ref[at])
    merge_s[...] = grad_merge
    head_s[...] = grad_head
    for apart, pack_out in enumerate((pack_0, pack_1, pack_2, pack_3)):
        quarter = lax.bitwise_xor(stream, jnp.int32(apart))
        for grad_s, base in ((merge_s, 0), (head_s, merge_rows)):
            share = grad_s.shape[0] // 4
            at = pl.ds(pl.multiple_of(quarter * share, share), share)
            for tile in range(4):
                to = base + tile * share
                pack_out[to : to + share] = grad_s[at, tile * LANES : (tile + 1) * LANES].astype(BF16)


def pair_kernel(same_ref, other_ref, *out_refs):
    for slot, out_ref in enumerate(out_refs):
        out_ref[...] = (same_ref[slot].astype(F32) + other_ref[slot].astype(F32)).astype(BF16)


def frames_kernel(x_ref, cot_ref, *refs):
    total_refs, out_ref = refs[:-1], refs[-1]
    for part in range(x_ref.shape[0] // 32):
        rows = slice(part * 32, part * 32 + 32)
        inputs = x_ref[rows].astype(F32)
        mean = jnp.mean(inputs, axis=-1, keepdims=True)
        centred = inputs - mean
        rate = lax.rsqrt(jnp.mean(centred * centred, axis=-1, keepdims=True) + EPS)
        hat = centred * rate
        grad = total_refs[0][rows].astype(F32)
        for total_ref in total_refs[1:]:
            grad = grad + total_ref[rows].astype(F32)
        plain = jnp.mean(grad, axis=-1, keepdims=True)
        along = jnp.mean(grad * hat, axis=-1, keepdims=True)
        out_ref[rows] = cot_ref[rows].astype(F32) + rate * (grad - plain - hat * along)


def add_kernel(*refs):
    out_ref = refs[-1]
    first = 0
    for at in range(0, len(refs) - 1, 4):
        total = refs[at][...].astype(F32)
        for ref in refs[at + 1 : at + 4]:
            total = total + ref[...].astype(F32)
        out_ref[first : first + total.shape[0]] = total.astype(BF16)
        first += total.shape[0]


def early_kernel(all_ref, qkv_out, pos_out, down_out, up_out):
    sources = all_ref.shape[0]
    share = HALF // (4 * sources)

    def lines_at(base, size):
        return jnp.concatenate([all_ref[source, base : base + size] for source in range(sources)], axis=0).astype(F32)

    for kind in range(4):
        lines = jnp.transpose(lines_at(kind * HEAD, HEAD))
        if kind < 3:
            qkv_out[:, kind * D : (kind + 1) * D] = lines
        else:
            pos_out[...] = lines
    for source in range(sources):
        for tile in range(4):
            at = 4 * HEAD + tile * share
            down_out[source * share : (source + 1) * share, tile * LANES : (tile + 1) * LANES] = all_ref[
                source, at : at + share
            ].astype(F32)
    wide = sources * share
    for group in range(4):
        up_out.buffer[:, group * wide : (group + 1) * wide] = jnp.transpose(
            lines_at(4 * HEAD + 4 * share + group * share, share)
        )


def late_kernel(*refs):
    part_refs = refs[1 : HEADS + 1]
    (
        attn_gain_out,
        attn_bias_out,
        mlp_gain_out,
        mlp_bias_out,
        content_out,
        position_out,
        outw_out,
        up_out,
        up_bias_out,
        gain_out,
        bias_out,
        taps_out,
        conv_bias_out,
        down_bias_out,
        merge_out,
        merge_bias_out,
        all_s,
    ) = refs[HEADS + 1 :]
    place = lax.axis_index("tm")
    sources = all_s.shape[0]
    for apart, part_ref in enumerate(part_refs):
        all_s[lax.bitwise_xor(jnp.int32(apart), place)] = part_ref[...]
    channels = HALF // sources
    share = channels // 4

    def lines_at(base, size):
        return jnp.concatenate([all_s[source, base : base + size] for source in range(sources)], axis=0).astype(F32)

    for group in range(4):
        at = group * sources * share
        up_out.buffer[:, at : at + sources * share] = jnp.transpose(lines_at(group * share, share))
    up_out.go()
    table = jnp.transpose(lines_at(channels, share))
    taps_out[...] = table[:KERNEL]
    conv_bias_out[...] = table[KERNEL]
    gain_out[...] = table[KERNEL + 1]
    bias_out[...] = table[KERNEL + 2]
    wide = sources * share
    up_bias_out[:wide] = table[KERNEL + 3]
    up_bias_out[wide:] = table[KERNEL + 4]
    base = channels + share
    lines = all_s[0, base : base + 16].astype(F32)
    for source in range(1, sources):
        lines = lines + all_s[source, base : base + 16].astype(F32)
    outs = (attn_gain_out, attn_bias_out, mlp_gain_out, mlp_bias_out, content_out, position_out, down_bias_out, merge_bias_out)
    for line, out in enumerate(outs):
        out[...] = lines[line]
    base = base + 16
    merge_share = 2 * D // (4 * sources)
    head_share = D // (4 * sources)
    for source in range(sources):
        for tile in range(4):
            lanes = slice(tile * LANES, (tile + 1) * LANES)
            at = base + tile * merge_share
            merge_out[source * merge_share : (source + 1) * merge_share, lanes] = all_s[
                source, at : at + merge_share
            ].astype(F32)
            at = base + 4 * merge_share + tile * head_share
            outw_out[source * head_share : (source + 1) * head_share, lanes] = all_s[
                source, at : at + head_share
            ].astype(F32)


def moved(block, axis, bits):
    count = lax.axis_size(axis)
    return lax.ppermute(block, axis, [(index, index ^ bits) for index in range(count)])


def spread(block):
    near = [block] + [moved(block, "tm", bits) for bits in range(2, lax.axis_size("tm"), 2)]
    far = [moved(part, "tm", 1) for part in near]
    return [part for pair in zip(near, far) for part in pair]


def head_device(
    frames,
    lengths,
    cotangent,
    ln_attn_gain,
    ln_attn_bias,
    ln_mlp_gain,
    ln_mlp_bias,
    qkv_weight,
    content_bias,
    position_bias,
    pos_weight,
    out_weight,
    up_weight,
    up_bias,
    gate_norm_gain,
    gate_norm_bias,
    conv_kernel,
    conv_bias,
    down_weight,
    down_bias,
    merge_weight,
    merge_bias,
):
    count = lax.axis_size("tm")
    quarters = lax.axis_size("stream")
    own = frames.shape[1]
    total = own * count
    folded = total + total // 2
    padded = folded + 4 * MARGIN
    share = HALF // (quarters * count)
    channels = HALF // count
    quarter = D // quarters
    own_frames = frames[0]
    own_cotangent = cotangent[0]

    whole, late = Part(), Part(late=True)
    blocks = spread(own_frames)
    cot = lax.all_gather(own_cotangent, "tm", axis=0, tiled=True)
    up_own, table, qkv_own, pos_own, bias_own = kernel_call(
        select_kernel,
        [
            ((D, 3 * LANES), BF16),
            ((2, 8 + KERNEL + 1, LANES), F32),
            ((D, 3 * LANES), BF16),
            ((D, LANES), BF16),
            ((8, LANES), F32),
        ],
        10 * "v",
        micros=4,
    )(
        up_weight,
        up_bias,
        gate_norm_gain,
        gate_norm_bias,
        conv_bias,
        conv_kernel,
        qkv_weight,
        pos_weight,
        content_bias,
        position_bias,
    )
    frequency = jnp.exp(jnp.arange(D // 2, dtype=F32) * (-2.0 * math.log(10000.0) / D))
    coarse = jnp.arange(0, total, BLOCK, dtype=F32)[:, None] * frequency[None]
    fine = jnp.arange(BLOCK, dtype=F32)[:, None] * frequency[None]
    coarse_table = jnp.concatenate([jnp.sin(coarse), jnp.cos(coarse)], axis=1)
    fine_table = jnp.concatenate([jnp.sin(fine), jnp.cos(fine)], axis=1)

    n_attn, n_mlp, hat, q_position, query, key, value, prob, attn, row_share, stats = kernel_call(
        attend_kernel,
        [
            ((total, D), BF16, 1),
            ((total, D), BF16, 1),
            ((total, D), BF16, 1),
            ((total, LANES), BF16, 1),
            ((total, LANES + D), BF16, 1),
            ((total, LANES + D), BF16, 1),
            ((total, LANES), BF16, 1),
            ((total, total), BF16, 1),
            ((total, LANES), F32, 1),
            ((total, LANES), F32, 1),
            ((total, LANES), F32, 1),
        ],
        [
            "s",
            blocks_part(),
            *"vvvvvvvvv",
            Part((D, HALF), lambda refs, buffer: [(refs[0].at[:, pl.ds(HALF, HALF)], buffer)], late=True),
            "v",
        ],
        [((BLOCK, HALF), F32)],
        bounds=True,
        micros=18,
    )(
        lengths,
        *blocks,
        ln_attn_gain,
        ln_attn_bias,
        ln_mlp_gain,
        ln_mlp_bias,
        qkv_own,
        pos_own,
        bias_own,
        coarse_table,
        fine_table,
        up_weight,
        up_bias,
    )

    def own_down(refs, buffer):
        place = lax.axis_index("tm")
        stride = HALF // quarters
        return [
            (
                refs[0].at[pl.ds(pl.multiple_of(part * stride + share * place, 16), share)],
                buffer.at[pl.ds(part * share, share)],
            )
            for part in range(quarters)
        ]

    mixed, gate_pre, grad_y, slope, gate_hat, early_pack, vectors, first_lines = kernel_call(
        mlp_first_kernel,
        [
            ((count, own + 16, 2 * LANES), BF16, 1),
            ((folded, LANES), BF16, 1),
            ((folded, LANES), BF16, 1),
            ((folded, LANES), BF16, 1),
            ((folded, LANES), BF16, 1),
            ((quarters, 8 * share, LANES), BF16, 1),
            ((channels, LANES), F32),
            ((8, D), F32),
        ],
        [
            "s",
            whole,
            "v",
            "v",
            whole,
            Part(late=True),
            rows_part(D, D, late=True),
            Part((2 * LANES, D), own_down, late=True),
            Part(late=True),
        ],
        [
            ((folded, LANES), F32),
            ((folded, LANES), F32),
            ((total, 2 * LANES), BF16),
            ((folded, LANES), F32),
            ((folded, LANES), F32),
            ((padded, LANES), F32),
            ((padded, LANES), F32),
            ((folded, LANES), F32),
            ((folded, LANES), F32),
            ((total, D), BF16),
            ((total, 2 * LANES), BF16),
            ((2, 32, 8, LANES), F32),
            ((2, 32, 8, LANES), F32),
            ((2, 32, 8, LANES), F32),
            ((total, LANES), F32),
            ((3, WINDOW + 2 * MARGIN, LANES), F32),
            ((3, WINDOW + 2 * MARGIN, LANES), F32),
        ],
        bounds=True,
        micros=20,
    )(lengths, n_mlp, up_own, table, stats, cot, merge_weight, down_weight, attn)
    mixed_own = lax.all_to_all(mixed, "tm", 0, 0, tiled=True)

    def own_head(refs, buffer):
        at = pl.ds(pl.multiple_of(lax.axis_index("tm") * HEAD, HEAD), HEAD)
        return [(refs[0].at[at], buffer.at[pl.ds(0, HEAD)])]

    branch, from_attn, head_pack, head_lines = kernel_call(
        attend_back_kernel,
        [
            ((total, D), BF16, 1),
            ((total, D), BF16, 1),
            ((quarters, 4 * HEAD + 8 * share, LANES), BF16, 1),
            ((8, D), F32),
        ],
        [
            whole,
            rows_part(0, D),
            Part((LANES, D), own_head),
            whole,
            late,
            late,
            late,
            late,
            "v",
            "v",
            late,
            Part((total, LANES), lambda refs, buffer: [(refs[0].at[:, pl.ds(0, LANES)], buffer)], late=True),
            late,
            late,
            late,
            late,
            "v",
            late,
        ],
        [
            ((total, LANES), BF16),
            ((total, total), BF16),
            ((total, D), BF16),
            ((total, 3 * LANES), BF16),
            ((4 * HEAD, D), F32),
        ],
        micros=14,
    )(
        cot,
        merge_weight,
        out_weight,
        row_share,
        value,
        attn,
        prob,
        key,
        coarse_table,
        fine_table,
        pos_own,
        query,
        n_attn,
        q_position,
        qkv_own,
        hat,
        ln_attn_gain,
        early_pack,
    )
    head_part = lax.psum_scatter(head_pack, "stream", scatter_dimension=0)
    out_rows, joined = kernel_call(
        output_kernel,
        [((own, D), BF16), ((count, 256, own), BF16)],
        "vvvvvvv",
        micros=3,
        megas=24,
    )(own_frames, mixed_own, out_weight, down_weight, down_bias, merge_weight, merge_bias)
    joined_all = lax.all_to_all(joined, "tm", 0, 0, tiled=True)
    from_attn, _ = lax.optimization_barrier((from_attn, joined))

    pack_rows = 5 * share + 16
    same, apart, *up_packs = kernel_call(
        mlp_second_kernel,
        [((count // 2, own, D), BF16, 1)] * 2 + [((pack_rows, LANES), BF16)] * quarters,
        [
            Part((count, 2 * total // BLOCK, 2 * LANES), lambda refs, buffer: [(refs[0].at[:, pl.ds(own, 2 * total // BLOCK)], buffer)]),
            *([whole] * 4),
            late,
            late,
            "v",
            late,
            late,
            *"vvv",
        ],
        [
            ((total, 3 * LANES), BF16),
            ((total, LANES), F32),
            ((2 * LANES, D), F32),
            ((16, D), F32),
            ((channels, LANES), F32),
        ],
        micros=10,
    )(
        mixed_own,
        gate_pre,
        grad_y,
        slope,
        gate_hat,
        up_own,
        hat,
        ln_mlp_gain,
        from_attn,
        n_mlp,
        vectors,
        first_lines,
        head_lines,
    )
    sibling = moved(apart, "tm", 1)
    up_parts = [up_packs[0]] + [moved(up_packs[bits], "stream", bits) for bits in range(1, quarters)]
    pairs = kernel_call(pair_kernel, [((own, D), BF16)] * (count // 2), "vv", micros=1, megas=24)(same, sibling)
    sums = [pairs[0]] + [moved(pairs[slot], "tm", 2 * slot) for slot in range(1, count // 2)]
    joined_all, head_part, _ = lax.optimization_barrier((joined_all, head_part, pairs[0]))
    head_all = lax.all_gather(head_part, "tm", axis=0)
    merge_rows = 3 * D // count
    merge_packs = kernel_call(
        merge_kernel,
        [((merge_rows, LANES), BF16)] * quarters,
        "vvv",
        [((2 * D // count, D), F32), ((D // count, D), F32)],
        micros=2,
        megas=24,
    )(joined_all, cot, branch)
    merge_parts = [merge_packs[0]] + [moved(merge_packs[bits], "stream", bits) for bits in range(1, quarters)]
    (late_part,) = kernel_call(
        add_kernel, [((pack_rows + merge_rows, LANES), BF16)], 2 * quarters * "v", micros=1, megas=24
    )(*up_parts, *merge_parts)
    late_parts = spread(late_part)
    (grad_frames,) = kernel_call(frames_kernel, [((own, D), F32)], (2 + count // 2) * "v", micros=1, megas=24)(
        own_frames, own_cotangent, *sums
    )
    grad_qkv, grad_pos, grad_down, half_up = kernel_call(
        early_kernel,
        [
            ((quarter, 3 * D), F32),
            ((quarter, D), F32),
            ((HALF // quarters, D), F32),
            ((quarter, 2 * HALF), F32, 1, (quarter, HALF), lambda ref: ref.at[:, pl.ds(0, HALF)]),
        ],
        "v",
        micros=2,
        megas=24,
    )(head_all)
    late = kernel_call(
        late_kernel,
        [((quarter,), F32)] * 6
        + [
            ((quarter, D), F32),
            ((quarter, 2 * HALF), F32, 1, (quarter, HALF), lambda ref: ref.at[:, pl.ds(HALF, HALF)]),
            ((2 * HALF // quarters,), F32),
            ((HALF // quarters,), F32),
            ((HALF // quarters,), F32),
            ((KERNEL, HALF // quarters), F32),
            ((HALF // quarters,), F32),
            ((quarter,), F32),
            ((2 * D // quarters, D), F32),
            ((quarter,), F32),
        ],
        "k" + count * "v",
        [((count,) + late_part.shape, BF16)],
        micros=2,
        megas=24,
        aliases={0: 7},
    )(half_up, *late_parts)
    return (
        (out_rows[None], grad_frames[None])
        + tuple(late[:4])
        + (grad_qkv,)
        + tuple(late[4:6])
        + (grad_pos,)
        + tuple(late[6:13])
        + (grad_down,)
        + tuple(late[13:])
    )


def per_device(*operands):
    fits = (
        lax.axis_size("tm") == HEADS
        and lax.axis_size("stream") * LANES == D
        and operands[0].shape[1] == BLOCK
    )
    return head_device(*operands) if fits else frame_device(*operands)


def solution(mesh):
    return jax.shard_map(
        per_device,
        mesh=mesh,
        in_specs=(
            P("stream", "tm", None),
            P("stream", None),
            P("stream", "tm", None),
            P(),
            P(),
            P(),
            P(),
            P(),
            P(),
            P(),
            P(),
            P(),
            P(),
            P(),
            P(),
            P(),
            P(),
            P(),
            P(),
            P(),
            P(),
            P(),
        ),
        out_specs=(
            P("stream", "tm", None),
            P("stream", "tm", None),
            P("stream"),
            P("stream"),
            P("stream"),
            P("stream"),
            P("stream", None),
            P("stream"),
            P("stream"),
            P("stream", None),
            P("stream", None),
            P("stream", None),
            P("stream"),
            P("stream"),
            P("stream"),
            P(None, "stream"),
            P("stream"),
            P("stream", None),
            P("stream"),
            P("stream", None),
            P("stream"),
        ),
        check_vma=False,
    )
```

```python
import math

import jax
import jax.numpy as jnp
from jax import lax
from jax.experimental import pallas as pl
from jax.experimental.pallas import tpu as pltpu
from jax.sharding import PartitionSpec as P

D = 512
HEADS = 8
HEAD = 64
KERNEL = 31
ITEMS = 5
HALF = 1536


EPS = 1e-05
MASKED = -1e30


def extended(block, sides, width):
    for axis, dim in sides:
        count = lax.axis_size(axis)
        forward = [(i, i + 1) for i in range(count - 1)]
        backward = [(target, source) for source, target in forward]
        low = lax.ppermute(
            lax.slice_in_dim(block, block.shape[dim] - width, None, axis=dim), axis, forward
        )
        high = lax.ppermute(lax.slice_in_dim(block, 0, width, axis=dim), axis, backward)
        block = jnp.concatenate([low, block, high], axis=dim)
    return block


def norm_rows(inputs, scale_row, shift_row):
    row_mean = jnp.mean(inputs, axis=-1, keepdims=True)
    centred = inputs - row_mean
    spread = jnp.mean(centred * centred, axis=-1, keepdims=True)
    return centred * lax.rsqrt(spread + EPS) * scale_row + shift_row


def gelu_exact(inputs):
    return jax.nn.gelu(inputs, approximate=False)


def frame_info(lengths, offset, extent):
    item_ends = jnp.cumsum(lengths)
    first_table = jnp.concatenate([item_ends - lengths, item_ends[-1:]])
    frame_index = offset + jnp.arange(extent, dtype=jnp.int32)
    item_of = jnp.sum((frame_index[:, None] >= item_ends[None, :]).astype(jnp.int32), axis=1)
    labels = jnp.arange(ITEMS + 1, dtype=jnp.int32)
    first_frame = jnp.sum(
        jnp.where(item_of[:, None] == labels[None, :], first_table[None, :], 0), axis=1
    )
    return (frame_index, item_of, frame_index - first_frame)


def angles(place_in):
    frequency = jnp.exp(jnp.arange(D // 2, dtype=jnp.float32) * (-2.0 * math.log(10000.0) / D))
    phase_angle = place_in.astype(jnp.float32)[:, None] * frequency[None, :]
    return (jnp.sin(phase_angle), jnp.cos(phase_angle))


def rel_query(projected, sine_rows, cosine_rows):
    half_size = projected.shape[-1] // 2
    first_half = projected[..., :half_size]
    second_half = projected[..., half_size:]
    sine_wide = sine_rows[:, None, :]
    cosine_wide = cosine_rows[:, None, :]
    return jnp.concatenate(
        [
            first_half * sine_wide + second_half * cosine_wide,
            second_half * sine_wide - first_half * cosine_wide,
        ],
        axis=-1,
    )


def step_size(extent):
    return math.gcd(extent, 512)


def score_block(q_content, q_rel, query_item, query_frame, key_block, key_start, lengths):
    extent = key_block.shape[0]
    key_frame, key_item, key_place = frame_info(lengths, key_start, extent)
    sine_rows, cosine_rows = angles(key_place)
    k_rel = jnp.concatenate([cosine_rows, sine_rows], axis=1).astype(jnp.bfloat16)
    raw_scores = jnp.einsum(
        "qhe,khe->hqk",
        q_content,
        key_block.reshape(extent, HEADS, HEAD),
        preferred_element_type=jnp.float32,
    )
    raw_scores = raw_scores + jnp.einsum(
        "qhc,kc->hqk", q_rel, k_rel, preferred_element_type=jnp.float32
    )
    allowed = (query_item[:, None] == key_item[None, :]) & (
        (query_item[:, None] < ITEMS) | (query_frame[:, None] == key_frame[None, :])
    )
    return (raw_scores, allowed, k_rel)


def block_grads(
    q_content,
    q_rel,
    query_item,
    query_frame,
    grad_out,
    log_total,
    delta_rows,
    key_block,
    value_block,
    key_start,
    lengths,
):
    extent = key_block.shape[0]
    raw_scores, allowed, k_rel = score_block(
        q_content, q_rel, query_item, query_frame, key_block, key_start, lengths
    )
    prob_rows = jnp.where(allowed[None], jnp.exp(raw_scores * 0.125 - log_total[:, :, None]), 0.0)
    grad_prob = jnp.einsum(
        "qhe,khe->hqk",
        grad_out,
        value_block.reshape(extent, HEADS, HEAD),
        preferred_element_type=jnp.float32,
    )
    grad_raw = (prob_rows * (grad_prob - delta_rows[:, :, None]) * 0.125).astype(jnp.bfloat16)
    return (prob_rows.astype(jnp.bfloat16), grad_raw, k_rel)


def frame_device(
    frames,
    lengths,
    cotangent,
    ln_attn_gain,
    ln_attn_bias,
    ln_mlp_gain,
    ln_mlp_bias,
    qkv_weight,
    content_bias,
    position_bias,
    pos_weight,
    out_weight,
    up_weight,
    up_bias,
    gate_norm_gain,
    gate_norm_bias,
    conv_kernel,
    conv_bias,
    down_weight,
    down_bias,
    merge_weight,
    merge_bias,
):
    row_count = frames.shape[1]
    cycle_size = lax.axis_size("tm")
    offset = lax.axis_index("tm") * row_count
    stream_lengths = lengths[0]
    inputs = frames[0].astype(jnp.float32)
    frame_index, item_of, place_in = frame_info(stream_lengths, offset, row_count)
    sine_rows, cosine_rows = angles(place_in)
    attn_norm, attn_pull = jax.vjp(
        norm_rows, inputs, ln_attn_gain.astype(jnp.float32), ln_attn_bias.astype(jnp.float32)
    )
    mlp_norm, mlp_pull = jax.vjp(
        norm_rows, inputs, ln_mlp_gain.astype(jnp.float32), ln_mlp_bias.astype(jnp.float32)
    )
    attn_norm_low = attn_norm.astype(jnp.bfloat16)
    mlp_norm_low = mlp_norm.astype(jnp.bfloat16)
    qkv_rows = jnp.dot(attn_norm_low, qkv_weight, preferred_element_type=jnp.float32)
    query_rows = qkv_rows[:, :D]
    key_rows = qkv_rows[:, D : 2 * D].astype(jnp.bfloat16)
    value_rows = qkv_rows[:, 2 * D :].astype(jnp.bfloat16)
    q_content = (query_rows + content_bias.astype(jnp.float32)).astype(jnp.bfloat16)
    q_position = (query_rows + position_bias.astype(jnp.float32)).astype(jnp.bfloat16)
    content_heads = q_content.reshape(row_count, HEADS, HEAD)
    position_heads = q_position.reshape(row_count, HEADS, HEAD)
    pos_heads = pos_weight.reshape(D, HEADS, HEAD)
    projected = jnp.einsum(
        "the,che->thc", position_heads, pos_heads, preferred_element_type=jnp.float32
    )
    q_rel = rel_query(projected, sine_rows, cosine_rows).astype(jnp.bfloat16)
    start_state = (
        jnp.full((HEADS, row_count), MASKED, jnp.float32),
        jnp.zeros((HEADS, row_count), jnp.float32),
        jnp.zeros((HEADS, row_count, HEAD), jnp.float32),
    )
    fold_state = start_state
    key_piece = lax.all_gather(key_rows, "tm", axis=0, tiled=True)
    value_piece = lax.all_gather(value_rows, "tm", axis=0, tiled=True)
    extent = key_piece.shape[0]
    step_rows = step_size(extent)

    def forward_one_step(inner_state, step_index):
        row_top, row_total, row_acc = inner_state
        key_block = lax.dynamic_slice_in_dim(key_piece, step_index * step_rows, step_rows, 0)
        value_block = lax.dynamic_slice_in_dim(value_piece, step_index * step_rows, step_rows, 0)
        raw_scores, allowed, k_rel = score_block(
            content_heads,
            q_rel,
            item_of,
            frame_index,
            key_block,
            step_index * step_rows,
            stream_lengths,
        )
        scaled = jnp.where(allowed[None], raw_scores * 0.125, MASKED)
        new_top = jnp.maximum(row_top, jnp.max(scaled, axis=2))
        weight = jnp.where(allowed[None], jnp.exp(scaled - new_top[:, :, None]), 0.0)
        factor = jnp.exp(row_top - new_top)
        row_total = row_total * factor + jnp.sum(weight, axis=2)
        row_acc = row_acc * factor[:, :, None] + jnp.einsum(
            "hqk,khe->hqe",
            weight.astype(jnp.bfloat16),
            value_block.reshape(step_rows, HEADS, HEAD),
            preferred_element_type=jnp.float32,
        )
        return ((new_top, row_total, row_acc), None)

    fold_state, unused = lax.scan(
        forward_one_step, fold_state, jnp.arange(extent // step_rows, dtype=jnp.int32)
    )
    row_top, row_total, row_acc = fold_state
    attn_heads = row_acc / row_total[:, :, None]
    log_total = row_top + jnp.log(row_total)
    attn_low = jnp.transpose(attn_heads, (1, 0, 2)).reshape(row_count, D).astype(jnp.bfloat16)
    branch_attn = jnp.dot(attn_low, out_weight, preferred_element_type=jnp.float32).astype(
        jnp.bfloat16
    )
    hidden_pre = jnp.dot(
        mlp_norm_low, up_weight, preferred_element_type=jnp.float32
    ) + up_bias.astype(jnp.float32)
    hidden, gelu_pull = jax.vjp(gelu_exact, hidden_pre)
    gate_half = hidden[:, :HALF]
    conv_norm, conv_pull = jax.vjp(
        norm_rows,
        hidden[:, HALF:],
        gate_norm_gain.astype(jnp.float32),
        gate_norm_bias.astype(jnp.float32),
    )
    conv_in = conv_norm.astype(jnp.bfloat16)
    half_width = KERNEL // 2
    conv_wide = extended(conv_in, (("tm", 0),), half_width)
    wide_frame, wide_item, wide_place = frame_info(
        stream_lengths, offset - half_width, row_count + 2 * half_width
    )
    kernel_rows = conv_kernel.astype(jnp.float32)
    conv_out = conv_bias.astype(jnp.float32) + jnp.zeros_like(gate_half)
    for tap_index in range(KERNEL):
        same_item = (wide_item[tap_index : tap_index + row_count] == item_of)[:, None]
        conv_out = (
            conv_out
            + jnp.where(
                same_item, conv_wide[tap_index : tap_index + row_count].astype(jnp.float32), 0.0
            )
            * kernel_rows[tap_index]
        )
    gated_low = (gate_half * conv_out).astype(jnp.bfloat16)
    branch_mlp = (
        jnp.dot(gated_low, down_weight, preferred_element_type=jnp.float32)
        + down_bias.astype(jnp.float32)
    ).astype(jnp.bfloat16)
    joined = jnp.concatenate([branch_attn, branch_mlp], axis=1)
    result = (
        inputs
        + jnp.dot(joined, merge_weight, preferred_element_type=jnp.float32)
        + merge_bias.astype(jnp.float32)
    )
    out_rows = result.astype(jnp.bfloat16)[None]
    grad_low = cotangent[0]
    grad_rows = grad_low.astype(jnp.float32)
    grad_merge_bias = jnp.sum(grad_rows, axis=0)
    grad_merge_weight = jnp.einsum(
        "tc,td->cd", joined, grad_low, preferred_element_type=jnp.float32
    )
    grad_joined = jnp.einsum(
        "td,cd->tc", grad_low, merge_weight, preferred_element_type=jnp.float32
    )
    grad_attn_branch = grad_joined[:, :D].astype(jnp.bfloat16)
    grad_mlp_branch = grad_joined[:, D:].astype(jnp.bfloat16)
    grad_down_weight = jnp.einsum(
        "tc,td->cd", gated_low, grad_mlp_branch, preferred_element_type=jnp.float32
    )
    grad_down_bias = jnp.sum(grad_mlp_branch.astype(jnp.float32), axis=0)
    grad_gated = jnp.einsum(
        "td,cd->tc", grad_mlp_branch, down_weight, preferred_element_type=jnp.float32
    )
    grad_gate_half = grad_gated * conv_out
    grad_conv_out = (grad_gated * gate_half).astype(jnp.bfloat16)
    grad_conv_rows = grad_conv_out.astype(jnp.float32)
    grad_conv_bias = jnp.sum(grad_conv_rows, axis=0)
    grad_wide = extended(grad_conv_out, (("tm", 0),), half_width)
    kernel_list = []
    grad_conv_in = jnp.zeros_like(grad_conv_rows)
    for tap_index in range(KERNEL):
        same_item = (wide_item[tap_index : tap_index + row_count] == item_of)[:, None]
        kernel_list.append(
            jnp.sum(
                jnp.where(
                    same_item, conv_wide[tap_index : tap_index + row_count].astype(jnp.float32), 0.0
                )
                * grad_conv_rows,
                axis=0,
            )
        )
        back_start = 2 * half_width - tap_index
        back_item = (wide_item[back_start : back_start + row_count] == item_of)[:, None]
        grad_conv_in = (
            grad_conv_in
            + jnp.where(
                back_item, grad_wide[back_start : back_start + row_count].astype(jnp.float32), 0.0
            )
            * kernel_rows[tap_index]
        )
    grad_conv_kernel = jnp.stack(kernel_list)
    grad_second, grad_gate_norm_gain, grad_gate_norm_bias = conv_pull(grad_conv_in)
    (grad_pre_rows,) = gelu_pull(jnp.concatenate([grad_gate_half, grad_second], axis=1))
    grad_pre = grad_pre_rows.astype(jnp.bfloat16)
    grad_up_bias = jnp.sum(grad_pre.astype(jnp.float32), axis=0)
    grad_up_weight = jnp.einsum(
        "tc,tf->cf", mlp_norm_low, grad_pre, preferred_element_type=jnp.float32
    )
    grad_mlp_norm = jnp.einsum("tf,cf->tc", grad_pre, up_weight, preferred_element_type=jnp.float32)
    grad_out_weight = jnp.einsum(
        "tc,td->cd", attn_low, grad_attn_branch, preferred_element_type=jnp.float32
    )
    grad_attn_low = jnp.einsum(
        "td,cd->tc", grad_attn_branch, out_weight, preferred_element_type=jnp.float32
    ).astype(jnp.bfloat16)
    grad_out_heads = grad_attn_low.reshape(row_count, HEADS, HEAD)
    delta_rows = jnp.sum(
        jnp.transpose(grad_out_heads.astype(jnp.float32), (1, 0, 2)) * attn_heads, axis=2
    )
    total_frames = row_count * cycle_size
    back_start_state = (
        jnp.zeros((row_count, HEADS, HEAD), jnp.float32),
        jnp.zeros((row_count, HEADS, D), jnp.float32),
        jnp.zeros((total_frames, D), jnp.float32),
        jnp.zeros((total_frames, D), jnp.float32),
    )
    back_key_piece = lax.all_gather(key_rows, "tm", axis=0, tiled=True)
    back_value_piece = lax.all_gather(value_rows, "tm", axis=0, tiled=True)
    extent = back_key_piece.shape[0]
    back_step_rows = step_size(extent)

    def back_one_step(inner_state, step_index):
        grad_content, grad_rel = inner_state
        key_block = lax.dynamic_slice_in_dim(
            back_key_piece, step_index * back_step_rows, back_step_rows, 0
        )
        value_block = lax.dynamic_slice_in_dim(
            back_value_piece, step_index * back_step_rows, back_step_rows, 0
        )
        prob_low, grad_raw, k_rel = block_grads(
            content_heads,
            q_rel,
            item_of,
            frame_index,
            grad_out_heads,
            log_total,
            delta_rows,
            key_block,
            value_block,
            step_index * back_step_rows,
            stream_lengths,
        )
        grad_content = grad_content + jnp.einsum(
            "hqk,khe->qhe",
            grad_raw,
            key_block.reshape(back_step_rows, HEADS, HEAD),
            preferred_element_type=jnp.float32,
        )
        grad_rel = grad_rel + jnp.einsum(
            "hqk,kc->qhc", grad_raw, k_rel, preferred_element_type=jnp.float32
        )
        key_part = jnp.einsum(
            "hqk,qhe->khe", grad_raw, content_heads, preferred_element_type=jnp.float32
        ).reshape(back_step_rows, D)
        value_part = jnp.einsum(
            "hqk,qhe->khe", prob_low, grad_out_heads, preferred_element_type=jnp.float32
        ).reshape(back_step_rows, D)
        return ((grad_content, grad_rel), (key_part, value_part))

    inner_state, block_parts = lax.scan(
        back_one_step,
        (back_start_state[0], back_start_state[1]),
        jnp.arange(extent // back_step_rows, dtype=jnp.int32),
    )
    key_all = block_parts[0].reshape(extent, D)
    value_all = block_parts[1].reshape(extent, D)
    grad_content, grad_rel, key_all, value_all = (
        inner_state[0],
        inner_state[1],
        key_all,
        value_all,
    )
    grad_keys, grad_values = (
        lax.psum_scatter(key_all, "tm", scatter_dimension=0, tiled=True),
        lax.psum_scatter(value_all, "tm", scatter_dimension=0, tiled=True),
    )
    half_size = D // 2
    rel_first = grad_rel[..., :half_size]
    rel_second = grad_rel[..., half_size:]
    sine_wide = sine_rows[:, None, :]
    cosine_wide = cosine_rows[:, None, :]
    grad_projected = jnp.concatenate(
        [
            rel_first * sine_wide - rel_second * cosine_wide,
            rel_first * cosine_wide + rel_second * sine_wide,
        ],
        axis=-1,
    ).astype(jnp.bfloat16)
    grad_pos_weight = jnp.einsum(
        "thc,the->che", grad_projected, position_heads, preferred_element_type=jnp.float32
    ).reshape(D, D)
    grad_q_position = jnp.einsum(
        "thc,che->the", grad_projected, pos_heads, preferred_element_type=jnp.float32
    )
    grad_content_bias = jnp.sum(grad_content, axis=0).reshape(D)
    grad_position_bias = jnp.sum(grad_q_position, axis=0).reshape(D)
    grad_query = (grad_content + grad_q_position).reshape(row_count, D).astype(jnp.bfloat16)
    grad_qkv = jnp.concatenate(
        [grad_query, grad_keys.astype(jnp.bfloat16), grad_values.astype(jnp.bfloat16)], axis=1
    )
    grad_qkv_weight = jnp.einsum(
        "tc,tf->cf", attn_norm_low, grad_qkv, preferred_element_type=jnp.float32
    )
    grad_attn_norm = jnp.einsum(
        "tf,cf->tc", grad_qkv, qkv_weight, preferred_element_type=jnp.float32
    )
    grad_from_attn, grad_ln_attn_gain, grad_ln_attn_bias = attn_pull(grad_attn_norm)
    grad_from_mlp, grad_ln_mlp_gain, grad_ln_mlp_bias = mlp_pull(grad_mlp_norm)
    grad_inputs = grad_rows + grad_from_attn + grad_from_mlp
    weight_grads = (
        grad_ln_attn_gain,
        grad_ln_attn_bias,
        grad_ln_mlp_gain,
        grad_ln_mlp_bias,
        grad_qkv_weight,
        grad_content_bias,
        grad_position_bias,
        grad_pos_weight,
        grad_out_weight,
        grad_up_weight,
        grad_up_bias,
        grad_gate_norm_gain,
        grad_gate_norm_bias,
        grad_conv_kernel,
        grad_conv_bias,
        grad_down_weight,
        grad_down_bias,
        grad_merge_weight,
        grad_merge_bias,
    )
    summed = lax.psum(
        (
            weight_grads[0],
            weight_grads[1],
            weight_grads[2],
            weight_grads[3],
            weight_grads[4],
            weight_grads[5],
            weight_grads[6],
            weight_grads[7],
            weight_grads[8],
            weight_grads[9],
            weight_grads[10],
            weight_grads[11],
            weight_grads[12],
            weight_grads[13],
            weight_grads[14],
            weight_grads[15],
            weight_grads[16],
            weight_grads[17],
            weight_grads[18],
        ),
        "tm",
    )
    shares = (
        lax.psum_scatter(
            summed[0].astype(jnp.bfloat16), "stream", scatter_dimension=0, tiled=True
        ).astype(jnp.float32),
        lax.psum_scatter(
            summed[1].astype(jnp.bfloat16), "stream", scatter_dimension=0, tiled=True
        ).astype(jnp.float32),
        lax.psum_scatter(
            summed[2].astype(jnp.bfloat16), "stream", scatter_dimension=0, tiled=True
        ).astype(jnp.float32),
        lax.psum_scatter(
            summed[3].astype(jnp.bfloat16), "stream", scatter_dimension=0, tiled=True
        ).astype(jnp.float32),
        lax.psum_scatter(
            summed[4].astype(jnp.bfloat16), "stream", scatter_dimension=0, tiled=True
        ).astype(jnp.float32),
        lax.psum_scatter(
            summed[5].astype(jnp.bfloat16), "stream", scatter_dimension=0, tiled=True
        ).astype(jnp.float32),
        lax.psum_scatter(
            summed[6].astype(jnp.bfloat16), "stream", scatter_dimension=0, tiled=True
        ).astype(jnp.float32),
        lax.psum_scatter(
            summed[7].astype(jnp.bfloat16), "stream", scatter_dimension=0, tiled=True
        ).astype(jnp.float32),
        lax.psum_scatter(
            summed[8].astype(jnp.bfloat16), "stream", scatter_dimension=0, tiled=True
        ).astype(jnp.float32),
        lax.psum_scatter(
            summed[9].astype(jnp.bfloat16), "stream", scatter_dimension=0, tiled=True
        ).astype(jnp.float32),
        lax.psum_scatter(
            summed[10].astype(jnp.bfloat16), "stream", scatter_dimension=0, tiled=True
        ).astype(jnp.float32),
        lax.psum_scatter(
            summed[11].astype(jnp.bfloat16), "stream", scatter_dimension=0, tiled=True
        ).astype(jnp.float32),
        lax.psum_scatter(
            summed[12].astype(jnp.bfloat16), "stream", scatter_dimension=0, tiled=True
        ).astype(jnp.float32),
        lax.psum_scatter(
            summed[13].astype(jnp.bfloat16), "stream", scatter_dimension=1, tiled=True
        ).astype(jnp.float32),
        lax.psum_scatter(
            summed[14].astype(jnp.bfloat16), "stream", scatter_dimension=0, tiled=True
        ).astype(jnp.float32),
        lax.psum_scatter(
            summed[15].astype(jnp.bfloat16), "stream", scatter_dimension=0, tiled=True
        ).astype(jnp.float32),
        lax.psum_scatter(
            summed[16].astype(jnp.bfloat16), "stream", scatter_dimension=0, tiled=True
        ).astype(jnp.float32),
        lax.psum_scatter(
            summed[17].astype(jnp.bfloat16), "stream", scatter_dimension=0, tiled=True
        ).astype(jnp.float32),
        lax.psum_scatter(
            summed[18].astype(jnp.bfloat16), "stream", scatter_dimension=0, tiled=True
        ).astype(jnp.float32),
    )
    return (out_rows, grad_inputs[None]) + tuple(shares)


LANES = 128
LOW = LANES // 2
BLOCK = 128
TALL = 256
WINDOW = 64
MARGIN = 16
BOUNDS = 16
MEGA = 1024 * 1024
F32 = jnp.float32
BF16 = jnp.bfloat16


def dot_nn(left, right):
    return jnp.dot(left, right, preferred_element_type=F32)


def dot_nt(left, right):
    return lax.dot_general(left, right, (((1,), (1,)), ((), ())), preferred_element_type=F32)


def dot_tn(left, right):
    return lax.dot_general(left, right, (((0,), (0,)), ((), ())), preferred_element_type=F32)


def rows_of(index, size, base=0):
    return pl.ds(pl.multiple_of(index * size, size) + base, size)


def line_of(ref):
    return ref[...].astype(F32).reshape(1, ref.shape[0])


def fold_rows(values):
    return jnp.sum(values.reshape(values.shape[0] // 8, 8, values.shape[1]), axis=0)


def one_row(values):
    return jnp.sum(values, axis=0, keepdims=True)


def turn(values):
    return pltpu.roll(values, LOW, 1)


def low_lanes(rows):
    return lax.broadcasted_iota(jnp.int32, (rows, LANES), 1) < LOW


def centre_rows(inputs):
    mean = jnp.mean(inputs, axis=-1, keepdims=True)
    centred = inputs - mean
    spread = jnp.mean(centred * centred, axis=-1, keepdims=True)
    return centred * lax.rsqrt(spread + EPS)


def gelu_parts(values):
    phi = 0.5 + 0.5 * lax.erf(values * math.sqrt(0.5))
    bell = jnp.exp(values * values * -0.5)
    return values * phi, phi + values * bell * (1.0 / math.sqrt(2.0 * math.pi))


class Part:
    def __init__(self, shape=None, pairs=None, refs=1, late=False):
        self.shape, self.pairs, self.refs, self.late = shape, pairs, refs, late

    def buffer(self, operand):
        return self.shape or operand.shape

    def copies(self, refs, buffer):
        return self.pairs(refs, buffer) if self.pairs else [(refs[0], buffer)]


def blocks_part(part, late=False):
    def pairs(refs, buffer):
        place = lax.axis_index("tm")
        return [
            (
                ref.at[:, pl.ds(part * D, D)],
                buffer.at[rows_of(lax.bitwise_xor(jnp.int32(apart), place), BLOCK)],
            )
            for apart, ref in enumerate(refs)
        ]

    return Part((HEADS * BLOCK, D), pairs, HEADS, late)


def rows_part(first, size, late=False):
    return Part((size, D), lambda refs, buffer: [(refs[0].at[pl.ds(first, size)], buffer)], late=late)


class Fetch:
    def __init__(self, pairs, buffer, sems, first):
        self.buffer, self.begun = buffer, False
        self.pending = [
            pltpu.make_async_copy(source, target, sems.at[first + index])
            for index, (source, target) in enumerate(pairs)
        ]

    def begin(self):
        if not self.begun:
            for copy in self.pending:
                copy.start()
        self.begun = True

    def __call__(self):
        self.begin()
        for copy in self.pending:
            copy.wait()
        self.pending = []
        return self.buffer


def begin(*fetches):
    for fetch in fetches:
        fetch.begin()


class Send:
    def __init__(self, buffer, target, sems):
        self.buffer, self.target, self.sems, self.copies = buffer, target, sems, []

    def go(self, *index):
        source, target = (self.buffer.at[index], self.target.at[index]) if index else (self.buffer, self.target)
        copy = pltpu.make_async_copy(source, target, self.sems[len(self.copies)])
        copy.start()
        self.copies.append(copy)

    def finish(self):
        if not self.copies:
            self.go()


SPACES = {"v": pltpu.VMEM, "s": pltpu.SMEM, "k": pl.ANY}


def kernel_call(body, out_shapes, plan, scratch=(), megas=58, bounds=False, aliases=None):
    def call(*operands):
        in_specs, buffers, at = [], [], 0
        for item in plan:
            if isinstance(item, Part):
                in_specs += [pl.BlockSpec(memory_space=pl.ANY)] * item.refs
                buffers.append(pltpu.VMEM(item.buffer(operands[at]), operands[at].dtype))
                at += item.refs
            else:
                in_specs.append(pl.BlockSpec(memory_space=SPACES[item]))
                at += 1
        sent = [out for out in out_shapes if len(out) > 2]
        buffers += [pltpu.VMEM(out[3] if len(out) > 3 else out[0], out[1]) for out in sent]
        sem_count = 64
        extra = [pltpu.SMEM((BOUNDS,), jnp.int32)] if bounds else []

        def outer(*refs):
            inputs, rest = refs[: len(in_specs)], refs[len(in_specs) :]
            outputs, rest = rest[: len(out_shapes)], rest[len(out_shapes) :]
            held, rest = list(rest[: len(buffers)]), rest[len(buffers) :]
            sems, rest = rest[0], rest[1:]
            given, at, used = [], 0, 0
            for item in plan:
                if isinstance(item, Part):
                    buffer = held.pop(0)
                    pairs = item.copies(inputs[at : at + item.refs], buffer)
                    given.append(Fetch(pairs, buffer, sems, used))
                    if not item.late:
                        given[-1].begin()
                    used += len(pairs)
                    at += item.refs
                else:
                    given.append(inputs[at])
                    at += 1
            results = []
            for out, ref in zip(out_shapes, outputs):
                if len(out) > 2:
                    target = out[4](ref) if len(out) > 3 else ref
                    results.append(Send(held.pop(0), target, [sems.at[used], sems.at[used + 1]]))
                    used += 2
                else:
                    results.append(ref)
            assert used <= sem_count
            body(*given, *results, *rest)
            for item in given:
                if isinstance(item, Fetch):
                    item()
            sends = [item for item in results if isinstance(item, Send)]
            for item in sends:
                item.finish()
            for item in sends:
                for copy in item.copies:
                    copy.wait()

        return pl.pallas_call(
            outer,
            out_shape=[jax.ShapeDtypeStruct(out[0], out[1]) for out in out_shapes],
            in_specs=in_specs,
            out_specs=[pl.BlockSpec(memory_space=pl.ANY if len(out) > 2 else pltpu.VMEM) for out in out_shapes],
            scratch_shapes=buffers
            + [pltpu.SemaphoreType.DMA((sem_count,))]
            + [pltpu.VMEM(shape, kind) for shape, kind in scratch]
            + extra,
            input_output_aliases=aliases or {},
            compiler_params=pltpu.CompilerParams(vmem_limit_bytes=megas * MEGA),
            cost_estimate=pl.CostEstimate(flops=0, bytes_accessed=0, transcendentals=0),
        )(*operands)

    return call


def fill_bounds(lengths_ref, bounds_s, total):
    bounds_s[0] = jnp.int32(0)
    end = jnp.int32(0)
    for item in range(ITEMS):
        end = end + lengths_ref[0, item]
        bounds_s[item + 1] = end
    for item in range(ITEMS + 1, BOUNDS):
        bounds_s[item] = jnp.int32(total)


def select_kernel(
    up_ref,
    up_bias_ref,
    gain_ref,
    bias_ref,
    conv_bias_ref,
    taps_ref,
    qkv_ref,
    pos_ref,
    content_ref,
    position_ref,
    up_out,
    table_out,
    qkv_out,
    pos_out,
    bias_out,
):
    place = lax.axis_index("tm")
    quarters = lax.axis_size("stream")
    share = HALF // (quarters * lax.axis_size("tm"))
    lane = lax.broadcasted_iota(jnp.int32, (1, 2 * LANES), 1)
    channel = jnp.where(lane < LANES + LOW, lane, lane - LOW)
    group = jnp.zeros_like(channel)
    for quarter in range(1, quarters):
        group = group + (channel >= quarter * share).astype(jnp.int32)
    source = group * (HALF // quarters) + share * place + channel - group * share
    chosen = (lax.broadcasted_iota(jnp.int32, (HALF, 2 * LANES), 0) == source).astype(F32).astype(BF16)
    gate = dot_nn(up_ref[:, :HALF], chosen)
    conv = dot_nn(up_ref[:, HALF:], chosen)
    up_out[:, :LANES] = gate[:, :LANES].astype(BF16)
    up_out[:, LANES : 2 * LANES] = jnp.where(low_lanes(D), gate[:, LANES:], conv[:, LANES:]).astype(BF16)
    up_out[:, 2 * LANES :] = conv[:, :LANES].astype(BF16)
    up_bias = line_of(up_bias_ref)
    lines = jnp.concatenate(
        [
            up_bias[:, :HALF],
            up_bias[:, HALF:],
            line_of(gain_ref),
            line_of(bias_ref),
            line_of(conv_bias_ref),
            jnp.zeros((3, HALF), F32),
        ],
        axis=0,
    )
    lines = dot_nn(lines.astype(BF16), chosen)
    taps = dot_nn(taps_ref[...], chosen)
    for part in range(2):
        lanes = slice(part * LANES, (part + 1) * LANES)
        table_out[part, :8] = lines[:, lanes]
        table_out[part, 8 : 8 + KERNEL] = taps[:, lanes]
        table_out[part, 8 + KERNEL :] = jnp.zeros((1, LANES), F32)

    odd = lax.rem(place, 2) == 1

    def head_lanes(ref, base):
        at = pl.ds(pl.multiple_of(lax.div(place, 2) * LANES + base, LANES), LANES)
        values = ref[:, at].astype(F32)
        values = jnp.where(odd, turn(values), values)
        return jnp.where(low_lanes(values.shape[0]), values, 0.0)

    for part in range(3):
        qkv_out[:, part * LANES : (part + 1) * LANES] = head_lanes(qkv_ref, part * D).astype(BF16)
    pos_out[...] = head_lanes(pos_ref, 0).astype(BF16)
    bias_out[...] = jnp.zeros((8, LANES), F32)
    for line, ref in enumerate((content_ref, position_ref)):
        values = line_of(ref)
        picked = values[:, :LANES]
        for tile in range(1, D // LANES):
            picked = jnp.where(
                lax.div(place, 2) == tile, values[:, tile * LANES : (tile + 1) * LANES], picked
            )
        picked = jnp.where(odd, turn(picked), picked)
        bias_out[line : line + 1] = jnp.where(low_lanes(1), picked, 0.0)


def angle_rows(coarse_ref, fine_ref, block, rows):
    half = D // 2
    base = coarse_ref[pl.ds(block, 1)]
    base_sine, base_cosine = base[:, :half], base[:, half:]
    sine, cosine = fine_ref[rows, :half], fine_ref[rows, half:]
    return base_sine * cosine + base_cosine * sine, base_cosine * cosine - base_sine * sine


def item_codes(bounds_s, index):
    code = jnp.zeros_like(index)
    for item in range(1, ITEMS + 1):
        code = code + (index >= bounds_s[item]).astype(jnp.int32)
    return jnp.where(code < ITEMS, code, ITEMS + index)


def attend_kernel(
    lengths_ref,
    x_ref,
    attn_gain_ref,
    attn_bias_ref,
    mlp_gain_ref,
    mlp_bias_ref,
    qkv_ref,
    pos_ref,
    bias_ref,
    coarse_ref,
    fine_ref,
    up_ref,
    up_bias_ref,
    n_attn_out,
    n_mlp_out,
    hat_out,
    q_position_out,
    query_out,
    key_out,
    value_out,
    prob_out,
    attn_out,
    share_out,
    stats_out,
    pre_s,
    bounds_s,
):
    frames = n_attn_out.buffer.shape[0]
    half = D // 2
    fill_bounds(lengths_ref, bounds_s, frames)
    attn_gain, attn_bias = line_of(attn_gain_ref), line_of(attn_bias_ref)
    mlp_gain, mlp_bias = line_of(mlp_gain_ref), line_of(mlp_bias_ref)
    content, position = bias_ref[0:1], bias_ref[1:2]
    x_ref = x_ref()
    begin(up_ref)

    @pl.loop(0, frames // TALL, unroll=2)
    def _(block):
        rows = rows_of(block, TALL)
        for part in range(TALL // 32):
            at = rows_of(block, TALL, part * 32)
            at = pl.ds(pl.multiple_of(block * TALL + part * 32, 32), 32)
            hat = centre_rows(x_ref[at].astype(F32))
            hat_out.buffer[at] = hat.astype(BF16)
            n_attn_out.buffer[at] = (hat * attn_gain + attn_bias).astype(BF16)
            n_mlp_out.buffer[at] = (hat * mlp_gain + mlp_bias).astype(BF16)
        parts = dot_nn(n_attn_out.buffer[rows], qkv_ref[...])
        query = parts[:, :LANES]
        query_out.buffer[rows, :LANES] = ((query + content).astype(BF16).astype(F32) * 0.125).astype(BF16)
        q_position = (query + position).astype(BF16)
        q_position_out.buffer[rows] = q_position
        key_out.buffer[rows, :LANES] = parts[:, LANES : 2 * LANES].astype(BF16)
        value_out.buffer[rows] = parts[:, 2 * LANES :].astype(BF16)
        projected = dot_nt(q_position, pos_ref[...])
        for part in range(TALL // 32):
            at = pl.ds(pl.multiple_of(block * TALL + part * 32, 32), 32)
            inner = part * 32 % BLOCK
            sine, cosine = angle_rows(
                coarse_ref, fine_ref, block * (TALL // BLOCK) + part * 32 // BLOCK, slice(inner, inner + 32)
            )
            first = projected[part * 32 : part * 32 + 32, :half]
            second = projected[part * 32 : part * 32 + 32, half:]
            query_out.buffer[at, LANES : LANES + half] = ((first * sine + second * cosine) * 0.125).astype(BF16)
            query_out.buffer[at, LANES + half :] = ((second * sine - first * cosine) * 0.125).astype(BF16)
            key_out.buffer[at, LANES : LANES + half] = cosine.astype(BF16)
            key_out.buffer[at, LANES + half :] = sine.astype(BF16)

    for out in (n_attn_out, n_mlp_out, hat_out, q_position_out, query_out, key_out, value_out):
        out.go()
    up_ref = up_ref()
    up_bias = line_of(up_bias_ref)[:, HALF:]
    lane = lax.broadcasted_iota(jnp.int32, (16, LANES), 1)

    @pl.loop(0, frames // BLOCK)
    def _(block):
        pre_s[...] = dot_nn(n_mlp_out.buffer[rows_of(block, BLOCK)], up_ref[...])
        for part in range(BLOCK // 16):
            pre = pre_s[part * 16 : part * 16 + 16] + up_bias
            hidden = pre * (0.5 + 0.5 * lax.erf(pre * math.sqrt(0.5)))
            mean = jnp.mean(hidden, axis=-1, keepdims=True)
            centred = hidden - mean
            rate = lax.rsqrt(jnp.mean(centred * centred, axis=-1, keepdims=True) + EPS)
            at = pl.ds(pl.multiple_of(block * BLOCK + part * 16, 16), 16)
            stats_out.buffer[at] = jnp.where(lane == 0, mean, rate)

    stats_out.go()
    key_code = item_codes(bounds_s, lax.broadcasted_iota(jnp.int32, (1, frames), 1))

    @pl.loop(0, frames // TALL, unroll=2)
    def _(block):
        rows = rows_of(block, TALL)
        raw = dot_nt(query_out.buffer[rows], key_out.buffer[...])
        for part in range(TALL // 32):
            start = block * TALL + part * 32
            at = pl.ds(pl.multiple_of(start, 32), 32)
            index = start + lax.broadcasted_iota(jnp.int32, (32, 1), 0)
            scaled = jnp.where(
                item_codes(bounds_s, index) == key_code, raw[part * 32 : part * 32 + 32], MASKED
            )
            weight = jnp.exp(scaled - jnp.max(scaled, axis=1, keepdims=True))
            prob_out.buffer[at] = weight.astype(BF16)
            share_out.buffer[at] = jnp.broadcast_to(1.0 / jnp.sum(weight, axis=1, keepdims=True), (32, LANES))
        attn_out.buffer[rows] = (
            dot_nn(prob_out.buffer[rows], value_out.buffer[...]) * share_out.buffer[rows]
        )


def fill_margins(wide_s, frames):
    edge = jnp.zeros((MARGIN, LANES), F32)
    wide_s[:MARGIN] = edge
    wide_s[MARGIN + frames : 2 * MARGIN + frames] = edge
    base = frames + 3 * MARGIN
    after = base + frames // 2
    low = low_lanes(MARGIN)
    wide_s[base - MARGIN : base] = jnp.where(low, 0.0, turn(wide_s[after - MARGIN : after]))
    wide_s[after : after + MARGIN] = jnp.where(low, turn(wide_s[base : base + MARGIN]), 0.0)


def item_span(bounds_s, frame):
    begin, end = bounds_s[0], bounds_s[BOUNDS - 1]
    for item in range(1, ITEMS + 1):
        edge = bounds_s[item]
        begin = jnp.where(frame >= edge, edge, begin)
    for item in range(ITEMS, 0, -1):
        edge = bounds_s[item]
        end = jnp.where(frame < edge, edge, end)
    return begin, end


def is_whole(bounds_s, start):
    begin, end = item_span(bounds_s, start)
    reach = KERNEL // 2
    low = (begin == 0) | (begin <= start - reach)
    high = (end == bounds_s[BOUNDS - 1]) | (end >= start + WINDOW + reach)
    return low & high & (end >= start + WINDOW)


def tap_limits(bounds_s, start):
    frame = start + lax.broadcasted_iota(jnp.int32, (WINDOW, LANES), 0)
    begin, end = item_span(bounds_s, frame)
    return begin - frame, end - frame


def grouped(values):
    return values.reshape(WINDOW // 8, 8, LANES)


def triple_places(step, frames):
    half = frames // 2
    return (
        pl.multiple_of(step * WINDOW, 2 * MARGIN),
        pl.multiple_of(step * WINDOW + half, 2 * MARGIN),
        pl.multiple_of(step * WINDOW + frames + 2 * MARGIN, 2 * MARGIN),
    )


def over_windows(bounds_s, frames, body):
    half = frames // 2

    @pl.loop(0, half // WINDOW)
    def _(step):
        start = step * WINDOW
        whole = is_whole(bounds_s, start) & is_whole(bounds_s, start + half)

        @pl.when(whole)
        def _():
            body(step, None)

        @pl.when(jnp.logical_not(whole))
        def _():
            first, second = tap_limits(bounds_s, start), tap_limits(bounds_s, start + half)
            low = low_lanes(WINDOW)
            rest = [jnp.where(low, one, other) for one, other in zip(first, second)]
            body(step, (first, second, rest))


def tap_view(window_ref, tap, limits):
    view = window_ref[tap + 1 : tap + 1 + WINDOW]
    if limits is not None:
        shift = tap - KERNEL // 2
        view = jnp.where((limits[0] <= shift) & (limits[1] > shift), view, 0.0)
    return grouped(view)


def mlp_first_kernel(
    lengths_ref,
    n_ref,
    up_ref,
    table_ref,
    stats_ref,
    cot_ref,
    merge_ref,
    down_ref,
    attn_ref,
    mixed_out,
    gate_pre_out,
    grad_out,
    rate_out,
    hat_out,
    early_out,
    vectors_out,
    lines_out,
    hat_s,
    slope_s,
    gate_s,
    hidden_s,
    gate_slope_s,
    conv_s,
    grad_s,
    out_s,
    back_s,
    branch_s,
    mix_s,
    taps_s,
    turn_s,
    tap_sum_s,
    columns_s,
    forward_s,
    backward_s,
    bounds_s,
):
    frames = mix_s.shape[0]
    half = frames // 2
    blocks = frames // BLOCK
    quarters, early_rows, _ = early_out.buffer.shape
    share = early_rows // 8
    channels = quarters * share
    fill_bounds(lengths_ref, bounds_s, frames)
    for part in range(2):
        for tap in range(KERNEL):
            line = jnp.broadcast_to(table_ref[part, 8 + tap : 9 + tap], (8, LANES))
            taps_s[part, tap] = line
            turn_s[part, KERNEL - 1 - tap] = line
    tap_sum_s[...] = jnp.zeros(tap_sum_s.shape, F32)
    main, rest = table_ref[0, :8], table_ref[1, :8]
    mixed_bias = jnp.where(low_lanes(1), rest[0:1], rest[1:2])
    low = low_lanes(64)
    gate_pre_ref = gate_pre_out.buffer
    n_ref = n_ref()
    stats_ref = stats_ref()
    begin(cot_ref, merge_ref, down_ref, attn_ref)

    def stat_rows(rows):
        stats = stats_ref[rows]
        return stats[:, 0:1], stats[:, 1:2]

    def chunk(start, base=0):
        return pl.ds(pl.multiple_of(start, 64) + base, 64)

    def conv_part(hidden, mean, rate, lines, rows, to_rows):
        hat = (hidden - mean) * rate
        hat_s[rows] = hat
        hat_out.buffer[rows] = hat.astype(BF16)
        conv_s[to_rows] = (hat * lines[2:3] + lines[3:4]).astype(BF16).astype(F32)

    @pl.loop(0, half // TALL)
    def _(block):
        pre = [dot_nn(n_ref[rows_of(block, TALL, base)], up_ref[...]) for base in (0, half)]
        for part in range(TALL // 64):
            inner = slice(part * 64, part * 64 + 64)
            start = block * TALL + part * 64
            mixed = []
            for values, base in zip(pre, (0, half)):
                rows = chunk(start, base)
                gate, gate_slope = gelu_parts(values[inner, :LANES] + main[0:1])
                hidden_s[rows] = gate
                gate_slope_s[rows] = gate_slope
                hidden, slope = gelu_parts(values[inner, 2 * LANES :] + main[1:2])
                mean, rate = stat_rows(rows)
                slope_s[rows] = slope * rate
                conv_part(hidden, mean, rate, main, rows, chunk(start, base + MARGIN))
                mixed.append((*gelu_parts(values[inner, LANES : 2 * LANES] + mixed_bias), mean, rate))
            (low_hidden, low_slope, low_mean, low_rate), (high_hidden, high_slope, high_mean, high_rate) = mixed
            rows = chunk(start, frames)
            hidden_s[rows] = jnp.where(low, low_hidden, turn(high_hidden))
            gate_slope_s[rows] = jnp.where(low, low_slope, turn(high_slope))
            rate = jnp.where(low, low_rate, high_rate)
            slope_s[rows] = jnp.where(low, turn(low_slope), high_slope) * rate
            conv_part(
                jnp.where(low, turn(low_hidden), high_hidden),
                jnp.where(low, low_mean, high_mean),
                rate,
                rest,
                rows,
                chunk(start, frames + 3 * MARGIN),
            )

    hat_out.go()
    fill_margins(conv_s, frames)
    tall = WINDOW + 2 * MARGIN
    outs = (0, half, frames)

    def convolve(step, limits):
        for index, base in enumerate(triple_places(step, frames)):
            forward_s[index] = conv_s[pl.ds(base, tall)]
        for index in range(3):
            own = None if limits is None else limits[index]
            total = jnp.zeros((WINDOW // 8, 8, LANES), F32)
            for tap in range(KERNEL):
                total = total + tap_view(forward_s.at[index], tap, own) * taps_s[index // 2, tap][None]
            lines = rest if index == 2 else main
            out_s[rows_of(step, WINDOW, outs[index])] = total.reshape(WINDOW, LANES) + lines[4:5]

    over_windows(bounds_s, frames, convolve)
    cot_ref = cot_ref()
    merge_ref = merge_ref()
    down_ref = down_ref()
    attn_ref = attn_ref()
    down_ref[channels:] = jnp.zeros((2 * LANES - channels, D), BF16)
    zero = jnp.zeros((8, LANES), F32)

    def branch_part(grad_gated, rows, to_rows, sums):
        up_sum, conv_sum = sums
        gate, conv = hidden_s[rows], out_s[rows]
        gate_pre = (grad_gated * conv * gate_slope_s[rows]).astype(BF16)
        gate_pre_ref[rows] = gate_pre
        grad_conv = (grad_gated * gate).astype(BF16).astype(F32)
        grad_s[to_rows] = grad_conv
        gate_pre = gate_pre.astype(F32)
        return gate * conv, gate_pre, (up_sum + fold_rows(gate_pre), conv_sum + fold_rows(grad_conv))

    def branch_step(block, sums):
        main_sums, rest_sums = sums
        grads = []
        for base in (0, half):
            rows = rows_of(block, TALL, base)
            branch = dot_nt(cot_ref[rows], merge_ref[...]).astype(BF16)
            branch_s[rows] = branch
            grads.append(dot_nt(branch, down_ref[...]))
        for part in range(TALL // 64):
            inner = slice(part * 64, part * 64 + 64)
            start = block * TALL + part * 64
            for values, base in zip(grads, (0, half)):
                rows = chunk(start, base)
                gated, gate_pre, main_sums = branch_part(
                    values[inner, :LANES], rows, chunk(start, base + MARGIN), main_sums
                )
                mix_s[rows, :LANES] = gated.astype(BF16)
                gate_s[rows, :LANES] = gate_pre.astype(BF16)
            grad = jnp.where(low, grads[0][inner, LANES:], turn(grads[1][inner, LANES:]))
            gated, gate_pre, rest_sums = branch_part(
                grad, chunk(start, frames), chunk(start, frames + 3 * MARGIN), rest_sums
            )
            low_rows, high_rows = chunk(start), chunk(start, half)
            gate_s[low_rows, LANES:] = gate_pre.astype(BF16)
            gate_s[high_rows, LANES:] = turn(gate_pre).astype(BF16)
            mix_s[low_rows, LANES:] = jnp.where(low, gated, turn(attn_ref[low_rows])).astype(BF16)
            mix_s[high_rows, LANES:] = jnp.where(low, turn(gated), turn(attn_ref[high_rows])).astype(BF16)
        return main_sums, rest_sums

    (main_up, main_conv), (rest_up, rest_conv) = lax.fori_loop(
        0, half // TALL, branch_step, ((zero, zero), (zero, zero))
    )
    gate_pre_out.go()
    fill_margins(grad_s, frames)
    ones = jnp.ones((16, frames), BF16)
    lines_out[0:1] = dot_nn(ones, branch_s[...])[0:1]
    lines_out[1:2] = dot_nn(ones, cot_ref[...])[0:1]
    lines_out[2:8] = jnp.zeros((6, D), F32)
    grad_down = dot_tn(mix_s[...], branch_s[...])
    grad_gate = dot_tn(gate_s[...], n_ref[...])
    for quarter in range(quarters):
        for tile in range(4):
            early_out.buffer[quarter, tile * share : (tile + 1) * share] = grad_down[
                quarter * share : (quarter + 1) * share, tile * LANES : (tile + 1) * LANES
            ].astype(BF16)
        early_out.buffer[quarter, 4 * share :] = grad_gate[
            :channels, quarter * LANES : (quarter + 1) * LANES
        ].astype(BF16)
    early_out.go()
    for block in range(blocks):
        mixed_out.buffer[block, :BLOCK] = mix_s[block * BLOCK : (block + 1) * BLOCK]
    mixed_out.go(slice(None), pl.ds(0, BLOCK))

    def differentiate(step, limits):
        for index, base in enumerate(triple_places(step, frames)):
            forward_s[index] = conv_s[pl.ds(base, tall)]
            backward_s[index] = grad_s[pl.ds(base, tall)]
        for index in range(3):
            own = None if limits is None else limits[index]
            total = jnp.zeros((WINDOW // 8, 8, LANES), F32)
            centre = grouped(backward_s[index, MARGIN : MARGIN + WINDOW])
            for tap in range(KERNEL):
                total = total + tap_view(backward_s.at[index], tap, own) * turn_s[index // 2, tap][None]
                tap_sum_s[index // 2, tap] += jnp.sum(tap_view(forward_s.at[index], tap, own) * centre, axis=0)
            back_s[rows_of(step, WINDOW, outs[index])] = total.reshape(WINDOW, LANES)

    over_windows(bounds_s, frames, differentiate)
    lane = lax.broadcasted_iota(jnp.int32, (64, LANES), 1)

    def norm_part(rows, lines, sums):
        gain_sum, bias_sum = sums
        back, hat, slope = back_s[rows], hat_s[rows], slope_s[rows]
        grad = back * lines[2:3]
        grad_out.buffer[rows] = (grad * slope).astype(BF16)
        rate_out.buffer[rows] = slope.astype(BF16)
        along = back * hat
        return grad, along * lines[2:3], (gain_sum + fold_rows(along), bias_sum + fold_rows(back))

    def norm_step(block, sums):
        main_sums, rest_sums = sums
        for part in range(TALL // 64):
            start = block * TALL + part * 64
            pairs = []
            for base in (0, half):
                plain, along, main_sums = norm_part(chunk(start, base), main, main_sums)
                pairs.append([plain, along])
            plain, along, rest_sums = norm_part(chunk(start, frames), rest, rest_sums)
            for item, values in enumerate((plain, along)):
                pairs[0][item] = pairs[0][item] + jnp.where(low, values, 0.0)
                pairs[1][item] = pairs[1][item] + jnp.where(low, 0.0, values)
            for (plain, along), base in zip(pairs, (0, half)):
                columns_s[chunk(start, base)] = jnp.where(
                    lane == 0,
                    jnp.sum(plain, axis=-1, keepdims=True),
                    jnp.where(lane == 1, jnp.sum(along, axis=-1, keepdims=True), 0.0),
                )
        return main_sums, rest_sums

    (main_gain, main_bias), (rest_gain, rest_bias) = lax.fori_loop(
        0, half // TALL, norm_step, ((zero, zero), (zero, zero))
    )
    grad_out.go()
    rate_out.go()
    totals = jnp.concatenate(
        [jnp.transpose(columns_s[block * BLOCK : (block + 1) * BLOCK])[:2] for block in range(blocks)], axis=0
    )
    high = totals.astype(BF16)
    low_part = (totals - high.astype(F32)).astype(BF16)
    for block in range(blocks):
        mixed_out.buffer[block, BLOCK:, :LANES] = high
        mixed_out.buffer[block, BLOCK:, LANES:] = low_part
    mixed_out.go(slice(None), pl.ds(BLOCK, 2 * blocks))

    def vectors(part, lines):
        taps = jnp.sum(tap_sum_s[part], axis=1)[:KERNEL]
        stacked = jnp.concatenate([taps] + [one_row(line) for line in lines], axis=0)
        if part:
            stacked = stacked + turn(stacked)
        return jnp.transpose(
            jnp.concatenate([stacked, jnp.zeros((LANES - stacked.shape[0], LANES), F32)], axis=0)
        )

    vectors_out[:LANES] = vectors(0, (main_conv, main_gain, main_bias, main_up))
    vectors_out[LANES:] = vectors(1, (rest_conv, rest_gain, rest_bias, rest_up))[: channels - LANES]


def attend_back_kernel(
    cot_ref,
    merge_ref,
    head_ref,
    share_ref,
    value_ref,
    attn_ref,
    prob_ref,
    key_ref,
    coarse_ref,
    fine_ref,
    pos_ref,
    query_ref,
    n_ref,
    q_position_ref,
    qkv_ref,
    hat_ref,
    gain_ref,
    early_ref,
    branch_out,
    total_out,
    pack_0,
    pack_1,
    pack_2,
    pack_3,
    lines_out,
    grad_s,
    raw_s,
    projected_s,
    parts_s,
    grads_s,
):
    place = lax.axis_index("tm")
    frames = raw_s.shape[0]
    blocks = frames // BLOCK
    half = D // 2
    zero = jnp.zeros((8, LANES), F32)
    cot_ref, merge_ref, head_ref, share_ref = cot_ref(), merge_ref(), head_ref(), share_ref()
    head_ref[HEAD:] = jnp.zeros((LANES - HEAD, D), BF16)
    begin(value_ref, attn_ref, prob_ref, key_ref, pos_ref)

    @pl.loop(0, frames // TALL, unroll=2)
    def _(block):
        rows = rows_of(block, TALL)
        branch = dot_nt(cot_ref[rows], merge_ref[...]).astype(BF16)
        branch_out.buffer[rows] = branch
        grad_s[rows] = (dot_nt(branch, head_ref[...]) * share_ref[rows]).astype(BF16)

    branch_out.go()
    value_ref, attn_ref, prob_ref = value_ref(), attn_ref(), prob_ref()
    key_ref, pos_ref = key_ref(), pos_ref()
    begin(query_ref, n_ref, q_position_ref, qkv_ref, hat_ref, early_ref)

    def score_step(block, sums):
        content_sum, position_sum = sums
        rows = rows_of(block, TALL)
        grad = grad_s[rows]
        score = dot_nt(grad, value_ref[...])
        for part in range(TALL // 32):
            at = pl.ds(pl.multiple_of(block * TALL + part * 32, 32), 32)
            inner = slice(part * 32, part * 32 + 32)
            delta = jnp.sum(grad[inner].astype(F32) * attn_ref[at], axis=1, keepdims=True)
            raw_s[at] = (prob_ref[at].astype(F32) * (score[inner] - delta)).astype(BF16)
        query = dot_nn(raw_s[rows], key_ref[...]) * 0.125
        for part in range(TALL // 32):
            at = pl.ds(pl.multiple_of(block * TALL + part * 32, 32), 32)
            inner = part * 32 % BLOCK
            sine, cosine = angle_rows(
                coarse_ref, fine_ref, block * (TALL // BLOCK) + part * 32 // BLOCK, slice(inner, inner + 32)
            )
            inner = slice(part * 32, part * 32 + 32)
            first, second = query[inner, LANES : LANES + half], query[inner, LANES + half :]
            projected_s[at, :half] = (first * sine - second * cosine).astype(BF16)
            projected_s[at, half:] = (first * cosine + second * sine).astype(BF16)
        position = dot_nn(projected_s[rows], pos_ref[...])
        content = query[:, :LANES]
        parts_s[rows, :LANES] = (content + position).astype(BF16)
        return content_sum + fold_rows(content), position_sum + fold_rows(position)

    content_sum, position_sum = lax.fori_loop(0, frames // TALL, score_step, (zero, zero), unroll=2)
    query_ref, n_ref, q_position_ref = query_ref(), n_ref(), q_position_ref()
    qkv_ref, hat_ref = qkv_ref(), hat_ref()
    grad_key = dot_tn(query_ref[...], raw_s[...])
    grad_value = dot_tn(grad_s[...], prob_ref[...])
    for block in range(blocks):
        at = slice(block * BLOCK, (block + 1) * BLOCK)
        parts_s[at, LANES : 2 * LANES] = jnp.transpose(grad_key[:, at]).astype(BF16)
        parts_s[at, 2 * LANES :] = jnp.transpose(grad_value[:, at]).astype(BF16)
    grads_s[:HEAD] = dot_tn(parts_s[:, :LANES], n_ref[...])[:HEAD]
    grads_s[HEAD : 2 * HEAD] = dot_nn(grad_key.astype(BF16), n_ref[...])[:HEAD]
    grads_s[2 * HEAD : 3 * HEAD] = dot_nn(grad_value.astype(BF16), n_ref[...])[:HEAD]
    grads_s[3 * HEAD :] = dot_tn(q_position_ref[...], projected_s[...])[:HEAD]
    stream = lax.axis_index("stream")
    early_ref = early_ref()
    for apart, pack_out in enumerate((pack_0, pack_1, pack_2, pack_3)):
        quarter = lax.bitwise_xor(stream, jnp.int32(apart))
        lanes = pl.ds(pl.multiple_of(quarter * LANES, LANES), LANES)
        pack_out.buffer[: 4 * HEAD] = grads_s[:, lanes].astype(BF16)
        pack_out.buffer[4 * HEAD :] = early_ref[quarter]
        pack_out.go()
    gain = line_of(gain_ref)
    wide_zero = jnp.zeros((8, D), F32)

    def norm_step(block, sums):
        gain_sum, bias_sum = sums
        grad = dot_nt(parts_s[rows_of(block, TALL)], qkv_ref[...])
        for part in range(TALL // 32):
            at = pl.ds(pl.multiple_of(block * TALL + part * 32, 32), 32)
            own = grad[part * 32 : part * 32 + 32]
            total_out.buffer[at] = (own * gain).astype(BF16)
            gain_sum = gain_sum + fold_rows(own * hat_ref[at].astype(F32))
            bias_sum = bias_sum + fold_rows(own)
        return gain_sum, bias_sum

    gain_sum, bias_sum = lax.fori_loop(0, frames // TALL, norm_step, (wide_zero, wide_zero), unroll=2)
    lane = lax.broadcasted_iota(jnp.int32, (1, LANES), 1)

    def own_lanes(sums):
        line = one_row(sums)
        line = line + turn(line)
        tiles = [
            jnp.where(lax.div(tile * LANES + lane, HEAD) == place, line, 0.0) for tile in range(D // LANES)
        ]
        return jnp.concatenate(tiles, axis=1)

    lines_out[...] = jnp.concatenate(
        [
            one_row(gain_sum),
            one_row(bias_sum),
            own_lanes(content_sum),
            own_lanes(position_sum),
            jnp.zeros((4, D), F32),
        ],
        axis=0,
    )


def mlp_second_kernel(
    mixed_ref,
    gate_pre_ref,
    grad_ref,
    rate_ref,
    hat_ref,
    n_ref,
    vectors_ref,
    pre_out,
    pack_0,
    pack_1,
    pack_2,
    pack_3,
    columns_s,
    grad_up_s,
    up_columns_s,
):
    packs = (pack_0, pack_1, pack_2, pack_3)
    stream = lax.axis_index("stream")
    pre_s = pre_out.buffer
    frames = pre_s.shape[0]
    half = frames // 2
    blocks = frames // BLOCK
    quarters = len(packs)
    channels = vectors_ref.shape[0]
    share = channels // quarters
    totals = jnp.zeros((2 * blocks, LANES), F32)
    mixed_ref = mixed_ref()
    for source in range(mixed_ref.shape[0]):
        both = mixed_ref[source].astype(F32)
        totals = totals + (both[:, :LANES] + both[:, LANES:])
    totals = totals * (1.0 / HALF)
    columns = jnp.transpose(jnp.concatenate([totals, jnp.zeros((LANES - 2 * blocks, LANES), F32)], axis=0))
    lane = lax.broadcasted_iota(jnp.int32, (BLOCK, LANES), 1)
    for block in range(blocks):
        columns_s[block * BLOCK : (block + 1) * BLOCK] = jnp.where(
            lane == 0, columns[:, 2 * block : 2 * block + 1], columns[:, 2 * block + 1 : 2 * block + 2]
        )
    gate_pre_ref, grad_ref, rate_ref, hat_ref = gate_pre_ref(), grad_ref(), rate_ref(), hat_ref()
    begin(n_ref)
    low = low_lanes(64)

    def chunk(start, base=0):
        return pl.ds(pl.multiple_of(start, 64) + base, 64)

    def pre_part(rows, table, up_sum):
        plain, along = table
        hat, rate = hat_ref[rows].astype(F32), rate_ref[rows].astype(F32)
        pre = (grad_ref[rows].astype(F32) - rate * (plain + hat * along)).astype(BF16).astype(F32)
        return pre, up_sum + fold_rows(pre)

    def pre_step(block, sums):
        main_up, rest_up = sums
        for part in range(TALL // 64):
            start = block * TALL + part * 64
            tables = []
            for base in (0, half):
                rows = chunk(start, base)
                values = columns_s[rows]
                table = [values[:, item : item + 1] for item in range(2)]
                tables.append(table)
                pre, main_up = pre_part(rows, table, main_up)
                pre_s[rows, :LANES] = gate_pre_ref[rows]
                pre_s[rows, 2 * LANES :] = pre.astype(BF16)
            rows = chunk(start, frames)
            table = [jnp.where(low, one, other) for one, other in zip(*tables)]
            pre, rest_up = pre_part(rows, table, rest_up)
            gate_pre = gate_pre_ref[rows].astype(F32)
            pre_s[chunk(start), LANES : 2 * LANES] = jnp.where(low, gate_pre, turn(pre)).astype(BF16)
            pre_s[chunk(start, half), LANES : 2 * LANES] = jnp.where(low, turn(gate_pre), pre).astype(BF16)
        return main_up, rest_up

    zero = jnp.zeros((8, LANES), F32)
    main_up, rest_up = lax.fori_loop(0, half // TALL, pre_step, (zero, zero))
    pre_out.go()
    n_ref = n_ref()
    grad_up_s[...] = dot_tn(pre_s[:, LANES:], n_ref[...])
    rest_line = one_row(rest_up)
    up_columns_s[:LANES] = jnp.transpose(jnp.broadcast_to(one_row(main_up), (LANES, LANES)))
    up_columns_s[LANES:] = jnp.transpose(jnp.broadcast_to(rest_line + turn(rest_line), (LANES, LANES)))[:LOW]
    gate_at = KERNEL + 3
    lane = lax.broadcasted_iota(jnp.int32, (share, LANES), 1)
    for apart, pack_out in enumerate(packs):
        quarter = lax.bitwise_xor(stream, jnp.int32(apart))
        lanes = pl.ds(pl.multiple_of(quarter * LANES, LANES), LANES)
        pack_out[:LANES] = grad_up_s[LANES:, lanes].astype(BF16)
        pack_out[LANES:channels] = grad_up_s[LOW:LANES, lanes].astype(BF16)
        table = vectors_ref[pl.ds(pl.multiple_of(quarter * share, 8), share)]
        for other in range(2):
            at = pl.ds(pl.multiple_of((2 * lax.rem(quarter, 2) + other) * share, 8), share)
            column = jnp.where(
                quarter < quarters // 2, vectors_ref[at][:, gate_at : gate_at + 1], up_columns_s[at][:, 0:1]
            )
            table = jnp.where(lane == gate_at + other, column, table)
        pack_out[channels:] = table.astype(BF16)


def merge_kernel(
    pre_ref,
    up_ref,
    norm_hat_ref,
    other_ref,
    joined_ref,
    branch_ref,
    cot_ref,
    gain_ref,
    first_lines_ref,
    head_lines_ref,
    same_out,
    apart_out,
    pack_0,
    pack_1,
    pack_2,
    pack_3,
    lines_s,
    merge_s,
    head_s,
):
    stream = lax.axis_index("stream")
    place = lax.axis_index("tm")
    pre_ref, up_ref = pre_ref(), up_ref()
    norm_hat_ref, other_ref = norm_hat_ref(), other_ref()
    begin(joined_ref, branch_ref, cot_ref)
    blocks = pre_ref.shape[0] // BLOCK
    gain = line_of(gain_ref)
    wide_zero = jnp.zeros((8, D), F32)

    def norm_step(block, sums):
        gain_sum, bias_sum = sums
        rows = rows_of(block, BLOCK)
        grad = dot_nt(pre_ref[rows], up_ref[...])
        total = (grad * gain + other_ref[rows].astype(F32)).astype(BF16)
        apart = lax.bitwise_xor(block, place)
        slot = lax.div(apart, 2)

        @pl.when(lax.rem(apart, 2) == 0)
        def _():
            same_out.buffer[slot] = total

        @pl.when(lax.rem(apart, 2) == 1)
        def _():
            apart_out.buffer[slot] = total

        return gain_sum + fold_rows(grad * norm_hat_ref[rows].astype(F32)), bias_sum + fold_rows(grad)

    gain_sum, bias_sum = lax.fori_loop(0, blocks, norm_step, (wide_zero, wide_zero), unroll=2)
    apart_out.go()
    same_out.go()
    first_device = (place == 0).astype(F32)
    lines_s[...] = jnp.concatenate(
        [
            head_lines_ref[0:2],
            one_row(gain_sum),
            one_row(bias_sum),
            head_lines_ref[2:4],
            first_lines_ref[0:2] * first_device,
            jnp.zeros((8, D), F32),
        ],
        axis=0,
    )
    joined_ref, branch_ref, cot_ref = joined_ref(), branch_ref(), cot_ref()
    sources, _, rows = joined_ref.shape
    merge_rows = merge_s.shape[0]
    head_rows = head_s.shape[0]
    grad_merge = jnp.zeros((merge_rows, D), F32)
    grad_head = jnp.zeros((head_rows, D), F32)
    for source in range(sources):
        at = slice(source * rows, (source + 1) * rows)
        joined = joined_ref[source]
        grad_merge = grad_merge + dot_nn(joined[:merge_rows], cot_ref[at])
        grad_head = grad_head + dot_nn(joined[merge_rows : merge_rows + head_rows], branch_ref[at])
    merge_s[...] = grad_merge
    head_s[...] = grad_head
    for apart, pack_out in enumerate((pack_0, pack_1, pack_2, pack_3)):
        quarter = lax.bitwise_xor(stream, jnp.int32(apart))
        for grad_s, base in ((merge_s, 0), (head_s, merge_rows)):
            share = grad_s.shape[0] // 4
            at = pl.ds(pl.multiple_of(quarter * share, share), share)
            for tile in range(4):
                to = base + tile * share
                pack_out[to : to + share] = grad_s[at, tile * LANES : (tile + 1) * LANES].astype(BF16)
        lanes = pl.ds(pl.multiple_of(quarter * LANES, LANES), LANES)
        pack_out[merge_rows + head_rows :] = lines_s[:, lanes].astype(BF16)


def output_kernel(
    x_ref, mixed_ref, head_ref, down_ref, down_bias_ref, merge_ref, merge_bias_ref, out_ref, joined_out
):
    sources = mixed_ref.shape[0]
    rows = x_ref.shape[0]
    channels = HALF // sources
    share = channels // 4
    attn_parts = []
    branch_attn = jnp.zeros((rows, D), F32)
    branch_mlp = jnp.zeros((rows, D), F32)
    for source in range(sources):
        attn = turn(mixed_ref[source, :rows, LANES:].astype(F32))[:, :HEAD].astype(BF16)
        attn_parts.append(attn)
        branch_attn = branch_attn + dot_nn(attn, head_ref[source * HEAD : (source + 1) * HEAD])
        down = jnp.concatenate(
            [down_ref[(part * sources + source) * share : (part * sources + source + 1) * share] for part in range(4)],
            axis=0,
        )
        branch_mlp = branch_mlp + dot_nn(mixed_ref[source, :rows, :channels], down)
    joined = jnp.concatenate(
        [branch_attn.astype(BF16), (branch_mlp + line_of(down_bias_ref)).astype(BF16)], axis=1
    )
    result = x_ref[...].astype(F32) + dot_nn(joined, merge_ref[...]) + line_of(merge_bias_ref)
    out_ref[...] = result.astype(BF16)
    turned = jnp.transpose(joined.astype(F32))
    heads = jnp.transpose(jnp.concatenate(attn_parts, axis=1).astype(F32))
    merge_share = turned.shape[0] // (4 * sources)
    head_share = heads.shape[0] // (4 * sources)
    used = 4 * (merge_share + head_share)
    for target in range(sources):
        for part in range(4):
            at = (part * sources + target) * merge_share
            joined_out[target, part * merge_share : (part + 1) * merge_share] = turned[
                at : at + merge_share
            ].astype(BF16)
            at = (part * sources + target) * head_share
            to = 4 * merge_share + part * head_share
            joined_out[target, to : to + head_share] = heads[at : at + head_share].astype(BF16)
        joined_out[target, used:] = jnp.zeros((joined_out.shape[1] - used, rows), BF16)


def pair_kernel(same_ref, other_ref, *out_refs):
    for slot, out_ref in enumerate(out_refs):
        out_ref[...] = (same_ref[slot].astype(F32) + other_ref[slot].astype(F32)).astype(BF16)


def frames_kernel(x_ref, cot_ref, *refs):
    total_refs, out_ref = refs[:-1], refs[-1]
    for part in range(x_ref.shape[0] // 32):
        rows = slice(part * 32, part * 32 + 32)
        inputs = x_ref[rows].astype(F32)
        mean = jnp.mean(inputs, axis=-1, keepdims=True)
        centred = inputs - mean
        rate = lax.rsqrt(jnp.mean(centred * centred, axis=-1, keepdims=True) + EPS)
        hat = centred * rate
        grad = total_refs[0][rows].astype(F32)
        for total_ref in total_refs[1:]:
            grad = grad + total_ref[rows].astype(F32)
        plain = jnp.mean(grad, axis=-1, keepdims=True)
        along = jnp.mean(grad * hat, axis=-1, keepdims=True)
        out_ref[rows] = cot_ref[rows].astype(F32) + rate * (grad - plain - hat * along)


def add_kernel(*refs):
    out_ref = refs[-1]
    first = 0
    for at in range(0, len(refs) - 1, 4):
        total = refs[at][...].astype(F32)
        for ref in refs[at + 1 : at + 4]:
            total = total + ref[...].astype(F32)
        out_ref[first : first + total.shape[0]] = total.astype(BF16)
        first += total.shape[0]


def gather_parts(part_refs, all_s):
    place = lax.axis_index("tm")
    for apart, part_ref in enumerate(part_refs):
        all_s[lax.bitwise_xor(jnp.int32(apart), place)] = part_ref[...]


def lines_from(all_s, base, size):
    return jnp.concatenate([all_s[source, base : base + size] for source in range(all_s.shape[0])], axis=0).astype(F32)


def early_kernel(*refs):
    qkv_out, pos_out, down_out, up_out, all_s = refs[HEADS:]
    gather_parts(refs[:HEADS], all_s)
    sources = all_s.shape[0]
    share = HALF // (4 * sources)
    for kind in range(4):
        lines = jnp.transpose(lines_from(all_s, kind * HEAD, HEAD))
        if kind < 3:
            qkv_out[:, kind * D : (kind + 1) * D] = lines
        else:
            pos_out[...] = lines
    base = 4 * HEAD
    for source in range(sources):
        for tile in range(4):
            down_out[source * share : (source + 1) * share, tile * LANES : (tile + 1) * LANES] = all_s[
                source, base + tile * share : base + (tile + 1) * share
            ].astype(F32)
    wide = sources * share
    for group in range(4):
        up_out.buffer[:, group * wide : (group + 1) * wide] = jnp.transpose(
            lines_from(all_s, base + 4 * share + group * share, share)
        )


def late_kernel(*refs):
    part_refs = refs[1 : HEADS + 1]
    (
        attn_gain_out,
        attn_bias_out,
        mlp_gain_out,
        mlp_bias_out,
        content_out,
        position_out,
        outw_out,
        up_out,
        up_bias_out,
        gain_out,
        bias_out,
        taps_out,
        conv_bias_out,
        down_bias_out,
        merge_out,
        merge_bias_out,
        all_s,
    ) = refs[HEADS + 1 :]
    gather_parts(part_refs, all_s)
    sources = all_s.shape[0]
    channels = HALF // sources
    share = channels // 4
    base = 0
    for group in range(4):
        at = group * sources * share
        up_out.buffer[:, at : at + sources * share] = jnp.transpose(lines_from(all_s, base + group * share, share))
    up_out.go()
    table = jnp.transpose(lines_from(all_s, base + channels, share))
    taps_out[...] = table[:KERNEL]
    conv_bias_out[...] = table[KERNEL]
    gain_out[...] = table[KERNEL + 1]
    bias_out[...] = table[KERNEL + 2]
    wide = sources * share
    up_bias_out[:wide] = table[KERNEL + 3]
    up_bias_out[wide:] = table[KERNEL + 4]
    base = base + channels + share
    merge_share = 2 * D // (4 * sources)
    head_share = D // (4 * sources)
    at = base + 4 * (merge_share + head_share)
    lines = all_s[0, at : at + 16].astype(F32)
    for source in range(1, sources):
        lines = lines + all_s[source, at : at + 16].astype(F32)
    outs = (attn_gain_out, attn_bias_out, mlp_gain_out, mlp_bias_out, content_out, position_out, down_bias_out, merge_bias_out)
    for line, out in enumerate(outs):
        out[...] = lines[line]
    for source in range(sources):
        for tile in range(4):
            lanes = slice(tile * LANES, (tile + 1) * LANES)
            at = base + tile * merge_share
            merge_out[source * merge_share : (source + 1) * merge_share, lanes] = all_s[
                source, at : at + merge_share
            ].astype(F32)
            at = base + 4 * merge_share + tile * head_share
            outw_out[source * head_share : (source + 1) * head_share, lanes] = all_s[
                source, at : at + head_share
            ].astype(F32)


def moved(block, axis, bits):
    count = lax.axis_size(axis)
    return lax.ppermute(block, axis, [(index, index ^ bits) for index in range(count)])


def over_streams(packs):
    return [packs[0]] + [moved(packs[bits], "stream", bits) for bits in range(1, lax.axis_size("stream"))]


def near_blocks(block):
    return [block] + [moved(block, "tm", bits) for bits in range(2, lax.axis_size("tm"), 2)]


def far_blocks(near):
    far = [moved(part, "tm", 1) for part in near]
    return [part for pair in zip(near, far) for part in pair]


def spread(block):
    return far_blocks(near_blocks(block))


def head_device(
    frames,
    lengths,
    cotangent,
    ln_attn_gain,
    ln_attn_bias,
    ln_mlp_gain,
    ln_mlp_bias,
    qkv_weight,
    content_bias,
    position_bias,
    pos_weight,
    out_weight,
    up_weight,
    up_bias,
    gate_norm_gain,
    gate_norm_bias,
    conv_kernel,
    conv_bias,
    down_weight,
    down_bias,
    merge_weight,
    merge_bias,
):
    count = lax.axis_size("tm")
    quarters = lax.axis_size("stream")
    own = frames.shape[1]
    total = own * count
    folded = total + total // 2
    padded = folded + 4 * MARGIN
    share = HALF // (quarters * count)
    channels = HALF // count
    quarter = D // quarters
    own_frames = frames[0]
    own_cotangent = cotangent[0]

    whole, late = Part(), Part(late=True)
    blocks = spread(jnp.concatenate([own_frames, own_cotangent], axis=1))
    up_own, table, qkv_own, pos_own, bias_own = kernel_call(
        select_kernel,
        [
            ((D, 3 * LANES), BF16),
            ((2, 8 + KERNEL + 1, LANES), F32),
            ((D, 3 * LANES), BF16),
            ((D, LANES), BF16),
            ((8, LANES), F32),
        ],
        10 * "v",
    )(
        up_weight,
        up_bias,
        gate_norm_gain,
        gate_norm_bias,
        conv_bias,
        conv_kernel,
        qkv_weight,
        pos_weight,
        content_bias,
        position_bias,
    )
    frequency = jnp.exp(jnp.arange(D // 2, dtype=F32) * (-2.0 * math.log(10000.0) / D))
    coarse = jnp.arange(0, total, BLOCK, dtype=F32)[:, None] * frequency[None]
    fine = jnp.arange(BLOCK, dtype=F32)[:, None] * frequency[None]
    coarse_table = jnp.concatenate([jnp.sin(coarse), jnp.cos(coarse)], axis=1)
    fine_table = jnp.concatenate([jnp.sin(fine), jnp.cos(fine)], axis=1)

    n_attn, n_mlp, hat, q_position, query, key, value, prob, attn, row_share, stats = kernel_call(
        attend_kernel,
        [
            ((total, D), BF16, 1),
            ((total, D), BF16, 1),
            ((total, D), BF16, 1),
            ((total, LANES), BF16, 1),
            ((total, LANES + D), BF16, 1),
            ((total, LANES + D), BF16, 1),
            ((total, LANES), BF16, 1),
            ((total, total), BF16, 1),
            ((total, LANES), F32, 1),
            ((total, LANES), F32, 1),
            ((total, LANES), F32, 1),
        ],
        [
            "s",
            blocks_part(0),
            *"vvvvvvvvv",
            Part((D, HALF), lambda refs, buffer: [(refs[0].at[:, pl.ds(HALF, HALF)], buffer)], late=True),
            "v",
        ],
        [((BLOCK, HALF), F32)],
        bounds=True,
    )(
        lengths,
        *blocks,
        ln_attn_gain,
        ln_attn_bias,
        ln_mlp_gain,
        ln_mlp_bias,
        qkv_own,
        pos_own,
        bias_own,
        coarse_table,
        fine_table,
        up_weight,
        up_bias,
    )

    def own_down(refs, buffer):
        place = lax.axis_index("tm")
        stride = HALF // quarters
        return [
            (
                refs[0].at[pl.ds(pl.multiple_of(part * stride + share * place, 16), share)],
                buffer.at[pl.ds(part * share, share)],
            )
            for part in range(quarters)
        ]

    mixed, gate_pre, grad_y, slope, gate_hat, early_pack, vectors, first_lines = kernel_call(
        mlp_first_kernel,
        [
            ((count, own + 16, 2 * LANES), BF16, 1),
            ((folded, LANES), BF16, 1),
            ((folded, LANES), BF16, 1),
            ((folded, LANES), BF16, 1),
            ((folded, LANES), BF16, 1),
            ((quarters, 8 * share, LANES), BF16, 1),
            ((channels, LANES), F32),
            ((8, D), F32),
        ],
        [
            "s",
            whole,
            "v",
            "v",
            whole,
            blocks_part(1, late=True),
            rows_part(D, D, late=True),
            Part((2 * LANES, D), own_down, late=True),
            Part(late=True),
        ],
        [
            ((folded, LANES), F32),
            ((folded, LANES), F32),
            ((total, 2 * LANES), BF16),
            ((folded, LANES), F32),
            ((folded, LANES), F32),
            ((padded, LANES), F32),
            ((padded, LANES), F32),
            ((folded, LANES), F32),
            ((folded, LANES), F32),
            ((total, D), BF16),
            ((total, 2 * LANES), BF16),
            ((2, 32, 8, LANES), F32),
            ((2, 32, 8, LANES), F32),
            ((2, 32, 8, LANES), F32),
            ((total, LANES), F32),
            ((3, WINDOW + 2 * MARGIN, LANES), F32),
            ((3, WINDOW + 2 * MARGIN, LANES), F32),
        ],
        bounds=True,
    )(lengths, n_mlp, up_own, table, stats, *blocks, merge_weight, down_weight, attn)
    mixed_own = lax.all_to_all(mixed, "tm", 0, 0, tiled=True)

    def own_head(refs, buffer):
        at = pl.ds(pl.multiple_of(lax.axis_index("tm") * HEAD, HEAD), HEAD)
        return [(refs[0].at[at], buffer.at[pl.ds(0, HEAD)])]

    branch, from_attn, *head_packs, head_lines = kernel_call(
        attend_back_kernel,
        [
            ((total, D), BF16, 1),
            ((total, D), BF16, 1),
            *([((4 * HEAD + 8 * share, LANES), BF16, 1)] * quarters),
            ((8, D), F32),
        ],
        [
            blocks_part(1),
            rows_part(0, D),
            Part((LANES, D), own_head),
            whole,
            late,
            late,
            late,
            late,
            "v",
            "v",
            late,
            Part((total, LANES), lambda refs, buffer: [(refs[0].at[:, pl.ds(0, LANES)], buffer)], late=True),
            late,
            late,
            late,
            late,
            "v",
            late,
        ],
        [
            ((total, LANES), BF16),
            ((total, total), BF16),
            ((total, D), BF16),
            ((total, 3 * LANES), BF16),
            ((4 * HEAD, D), F32),
        ],
    )(
        *blocks,
        merge_weight,
        out_weight,
        row_share,
        value,
        attn,
        prob,
        key,
        coarse_table,
        fine_table,
        pos_own,
        query,
        n_attn,
        q_position,
        qkv_own,
        hat,
        ln_attn_gain,
        early_pack,
    )
    head_parts = over_streams(head_packs)
    mixed_own, _ = lax.optimization_barrier((mixed_own, head_lines))
    out_rows, joined = kernel_call(
        output_kernel,
        [((own, D), BF16), ((count, 256, own), BF16)],
        "vvvvvvv",
        megas=24,
    )(own_frames, mixed_own, out_weight, down_weight, down_bias, merge_weight, merge_bias)
    joined_all = lax.all_to_all(joined, "tm", 0, 0, tiled=True)
    gate_pre, _ = lax.optimization_barrier((gate_pre, joined))
    up_rows = 5 * share
    pre, *up_packs = kernel_call(
        mlp_second_kernel,
        [((total, 3 * LANES), BF16, 1)] + [((up_rows, LANES), BF16)] * quarters,
        [
            Part(
                (count, 2 * total // BLOCK, 2 * LANES),
                lambda refs, buffer: [(refs[0].at[:, pl.ds(own, 2 * total // BLOCK)], buffer)],
            ),
            *([whole] * 4),
            late,
            "v",
        ],
        [((total, LANES), F32), ((2 * LANES, D), F32), ((channels, LANES), F32)],
    )(mixed_own, gate_pre, grad_y, slope, gate_hat, n_mlp, vectors)
    up_parts = over_streams(up_packs)
    head_parts, up_packs = lax.optimization_barrier((head_parts, up_packs))
    (early_part,) = kernel_call(add_kernel, [((4 * HEAD + 8 * share, LANES), BF16)], quarters * "v", megas=24)(
        *head_parts
    )
    pre, joined_all, early_part = lax.optimization_barrier((pre, joined_all, early_part))
    early_near = near_blocks(early_part)

    merge_rows = 3 * D // count + 16
    same, apart, *merge_packs = kernel_call(
        merge_kernel,
        [((count // 2, own, D), BF16, 1)] * 2 + [((merge_rows, LANES), BF16)] * quarters,
        [whole, whole, whole, whole, late, late, blocks_part(1, late=True), *"vvv"],
        [((16, D), F32), ((2 * D // count, D), F32), ((D // count, D), F32)],
    )(
        pre,
        up_own,
        hat,
        from_attn,
        joined_all,
        branch,
        *blocks,
        ln_mlp_gain,
        first_lines,
        head_lines,
    )
    apart, up_parts, early_near = lax.optimization_barrier((apart, up_parts, early_near))
    sibling = moved(apart, "tm", 1)
    merge_parts = over_streams(merge_packs)
    early_all = far_blocks(early_near)
    pairs = kernel_call(pair_kernel, [((own, D), BF16)] * (count // 2), "vv", megas=24)(same, sibling)
    sums = [pairs[0]] + [moved(pairs[slot], "tm", 2 * slot) for slot in range(1, count // 2)]
    merge_parts, early_all, sums = lax.optimization_barrier((merge_parts, early_all, sums))
    (late_part,) = kernel_call(add_kernel, [((up_rows + merge_rows, LANES), BF16)], 2 * quarters * "v", megas=24)(
        *up_parts, *merge_parts
    )
    late_parts = spread(late_part)
    (grad_frames,) = kernel_call(frames_kernel, [((own, D), F32)], (2 + count // 2) * "v", megas=24)(
        own_frames, own_cotangent, *sums
    )
    grad_qkv, grad_pos, grad_down, half_up = kernel_call(
        early_kernel,
        [
            ((quarter, 3 * D), F32),
            ((quarter, D), F32),
            ((HALF // quarters, D), F32),
            ((quarter, 2 * HALF), F32, 1, (quarter, HALF), lambda ref: ref.at[:, pl.ds(0, HALF)]),
        ],
        count * "v",
        [((count, 4 * HEAD + 8 * share, LANES), BF16)],
        megas=24,
    )(*early_all)
    late = kernel_call(
        late_kernel,
        [((quarter,), F32)] * 6
        + [
            ((quarter, D), F32),
            ((quarter, 2 * HALF), F32, 1, (quarter, HALF), lambda ref: ref.at[:, pl.ds(HALF, HALF)]),
            ((2 * HALF // quarters,), F32),
            ((HALF // quarters,), F32),
            ((HALF // quarters,), F32),
            ((KERNEL, HALF // quarters), F32),
            ((HALF // quarters,), F32),
            ((quarter,), F32),
            ((2 * D // quarters, D), F32),
            ((quarter,), F32),
        ],
        "k" + count * "v",
        [((count,) + late_part.shape, BF16)],
        megas=24,
        aliases={0: 7},
    )(half_up, *late_parts)
    return (
        out_rows[None],
        grad_frames[None],
        *late[:4],
        grad_qkv,
        *late[4:6],
        grad_pos,
        *late[6:13],
        grad_down,
        *late[13:],
    )


def per_device(*operands):
    fits = (
        lax.axis_size("tm") == HEADS
        and lax.axis_size("stream") * LANES == D
        and operands[0].shape[1] == BLOCK
    )
    return head_device(*operands) if fits else frame_device(*operands)


def solution(mesh):
    return jax.shard_map(
        per_device,
        mesh=mesh,
        in_specs=(
            P("stream", "tm", None),
            P("stream", None),
            P("stream", "tm", None),
            P(),
            P(),
            P(),
            P(),
            P(),
            P(),
            P(),
            P(),
            P(),
            P(),
            P(),
            P(),
            P(),
            P(),
            P(),
            P(),
            P(),
            P(),
            P(),
        ),
        out_specs=(
            P("stream", "tm", None),
            P("stream", "tm", None),
            P("stream"),
            P("stream"),
            P("stream"),
            P("stream"),
            P("stream", None),
            P("stream"),
            P("stream"),
            P("stream", None),
            P("stream", None),
            P("stream", None),
            P("stream"),
            P("stream"),
            P("stream"),
            P(None, "stream"),
            P("stream"),
            P("stream", None),
            P("stream"),
            P("stream", None),
            P("stream"),
        ),
        check_vma=False,
    )
```

```python
import math

import jax
import jax.numpy as jnp
from jax import lax
from jax.experimental import pallas as pl
from jax.experimental.pallas import tpu as pltpu
from jax.sharding import PartitionSpec as P

D = 512
HEADS = 8
HEAD = 64
KERNEL = 31
ITEMS = 5
HALF = 1536


EPS = 1e-05
MASKED = -1e30


def extended(block, sides, width):
    for axis, dim in sides:
        count = lax.axis_size(axis)
        forward = [(i, i + 1) for i in range(count - 1)]
        backward = [(target, source) for source, target in forward]
        low = lax.ppermute(
            lax.slice_in_dim(block, block.shape[dim] - width, None, axis=dim), axis, forward
        )
        high = lax.ppermute(lax.slice_in_dim(block, 0, width, axis=dim), axis, backward)
        block = jnp.concatenate([low, block, high], axis=dim)
    return block


def norm_rows(inputs, scale_row, shift_row):
    row_mean = jnp.mean(inputs, axis=-1, keepdims=True)
    centred = inputs - row_mean
    spread = jnp.mean(centred * centred, axis=-1, keepdims=True)
    return centred * lax.rsqrt(spread + EPS) * scale_row + shift_row


def gelu_exact(inputs):
    return jax.nn.gelu(inputs, approximate=False)


def frame_info(lengths, offset, extent):
    item_ends = jnp.cumsum(lengths)
    first_table = jnp.concatenate([item_ends - lengths, item_ends[-1:]])
    frame_index = offset + jnp.arange(extent, dtype=jnp.int32)
    item_of = jnp.sum((frame_index[:, None] >= item_ends[None, :]).astype(jnp.int32), axis=1)
    labels = jnp.arange(ITEMS + 1, dtype=jnp.int32)
    first_frame = jnp.sum(
        jnp.where(item_of[:, None] == labels[None, :], first_table[None, :], 0), axis=1
    )
    return (frame_index, item_of, frame_index - first_frame)


def angles(place_in):
    frequency = jnp.exp(jnp.arange(D // 2, dtype=jnp.float32) * (-2.0 * math.log(10000.0) / D))
    phase_angle = place_in.astype(jnp.float32)[:, None] * frequency[None, :]
    return (jnp.sin(phase_angle), jnp.cos(phase_angle))


def rel_query(projected, sine_rows, cosine_rows):
    half_size = projected.shape[-1] // 2
    first_half = projected[..., :half_size]
    second_half = projected[..., half_size:]
    sine_wide = sine_rows[:, None, :]
    cosine_wide = cosine_rows[:, None, :]
    return jnp.concatenate(
        [
            first_half * sine_wide + second_half * cosine_wide,
            second_half * sine_wide - first_half * cosine_wide,
        ],
        axis=-1,
    )


def step_size(extent):
    return math.gcd(extent, 512)


def score_block(q_content, q_rel, query_item, query_frame, key_block, key_start, lengths):
    extent = key_block.shape[0]
    key_frame, key_item, key_place = frame_info(lengths, key_start, extent)
    sine_rows, cosine_rows = angles(key_place)
    k_rel = jnp.concatenate([cosine_rows, sine_rows], axis=1).astype(jnp.bfloat16)
    raw_scores = jnp.einsum(
        "qhe,khe->hqk",
        q_content,
        key_block.reshape(extent, HEADS, HEAD),
        preferred_element_type=jnp.float32,
    )
    raw_scores = raw_scores + jnp.einsum(
        "qhc,kc->hqk", q_rel, k_rel, preferred_element_type=jnp.float32
    )
    allowed = (query_item[:, None] == key_item[None, :]) & (
        (query_item[:, None] < ITEMS) | (query_frame[:, None] == key_frame[None, :])
    )
    return (raw_scores, allowed, k_rel)


def block_grads(
    q_content,
    q_rel,
    query_item,
    query_frame,
    grad_out,
    log_total,
    delta_rows,
    key_block,
    value_block,
    key_start,
    lengths,
):
    extent = key_block.shape[0]
    raw_scores, allowed, k_rel = score_block(
        q_content, q_rel, query_item, query_frame, key_block, key_start, lengths
    )
    prob_rows = jnp.where(allowed[None], jnp.exp(raw_scores * 0.125 - log_total[:, :, None]), 0.0)
    grad_prob = jnp.einsum(
        "qhe,khe->hqk",
        grad_out,
        value_block.reshape(extent, HEADS, HEAD),
        preferred_element_type=jnp.float32,
    )
    grad_raw = (prob_rows * (grad_prob - delta_rows[:, :, None]) * 0.125).astype(jnp.bfloat16)
    return (prob_rows.astype(jnp.bfloat16), grad_raw, k_rel)


def frame_device(
    frames,
    lengths,
    cotangent,
    ln_attn_gain,
    ln_attn_bias,
    ln_mlp_gain,
    ln_mlp_bias,
    qkv_weight,
    content_bias,
    position_bias,
    pos_weight,
    out_weight,
    up_weight,
    up_bias,
    gate_norm_gain,
    gate_norm_bias,
    conv_kernel,
    conv_bias,
    down_weight,
    down_bias,
    merge_weight,
    merge_bias,
):
    row_count = frames.shape[1]
    cycle_size = lax.axis_size("tm")
    offset = lax.axis_index("tm") * row_count
    stream_lengths = lengths[0]
    inputs = frames[0].astype(jnp.float32)
    frame_index, item_of, place_in = frame_info(stream_lengths, offset, row_count)
    sine_rows, cosine_rows = angles(place_in)
    attn_norm, attn_pull = jax.vjp(
        norm_rows, inputs, ln_attn_gain.astype(jnp.float32), ln_attn_bias.astype(jnp.float32)
    )
    mlp_norm, mlp_pull = jax.vjp(
        norm_rows, inputs, ln_mlp_gain.astype(jnp.float32), ln_mlp_bias.astype(jnp.float32)
    )
    attn_norm_low = attn_norm.astype(jnp.bfloat16)
    mlp_norm_low = mlp_norm.astype(jnp.bfloat16)
    qkv_rows = jnp.dot(attn_norm_low, qkv_weight, preferred_element_type=jnp.float32)
    query_rows = qkv_rows[:, :D]
    key_rows = qkv_rows[:, D : 2 * D].astype(jnp.bfloat16)
    value_rows = qkv_rows[:, 2 * D :].astype(jnp.bfloat16)
    q_content = (query_rows + content_bias.astype(jnp.float32)).astype(jnp.bfloat16)
    q_position = (query_rows + position_bias.astype(jnp.float32)).astype(jnp.bfloat16)
    content_heads = q_content.reshape(row_count, HEADS, HEAD)
    position_heads = q_position.reshape(row_count, HEADS, HEAD)
    pos_heads = pos_weight.reshape(D, HEADS, HEAD)
    projected = jnp.einsum(
        "the,che->thc", position_heads, pos_heads, preferred_element_type=jnp.float32
    )
    q_rel = rel_query(projected, sine_rows, cosine_rows).astype(jnp.bfloat16)
    start_state = (
        jnp.full((HEADS, row_count), MASKED, jnp.float32),
        jnp.zeros((HEADS, row_count), jnp.float32),
        jnp.zeros((HEADS, row_count, HEAD), jnp.float32),
    )
    fold_state = start_state
    key_piece = lax.all_gather(key_rows, "tm", axis=0, tiled=True)
    value_piece = lax.all_gather(value_rows, "tm", axis=0, tiled=True)
    extent = key_piece.shape[0]
    step_rows = step_size(extent)

    def forward_one_step(inner_state, step_index):
        row_top, row_total, row_acc = inner_state
        key_block = lax.dynamic_slice_in_dim(key_piece, step_index * step_rows, step_rows, 0)
        value_block = lax.dynamic_slice_in_dim(value_piece, step_index * step_rows, step_rows, 0)
        raw_scores, allowed, k_rel = score_block(
            content_heads,
            q_rel,
            item_of,
            frame_index,
            key_block,
            step_index * step_rows,
            stream_lengths,
        )
        scaled = jnp.where(allowed[None], raw_scores * 0.125, MASKED)
        new_top = jnp.maximum(row_top, jnp.max(scaled, axis=2))
        weight = jnp.where(allowed[None], jnp.exp(scaled - new_top[:, :, None]), 0.0)
        factor = jnp.exp(row_top - new_top)
        row_total = row_total * factor + jnp.sum(weight, axis=2)
        row_acc = row_acc * factor[:, :, None] + jnp.einsum(
            "hqk,khe->hqe",
            weight.astype(jnp.bfloat16),
            value_block.reshape(step_rows, HEADS, HEAD),
            preferred_element_type=jnp.float32,
        )
        return ((new_top, row_total, row_acc), None)

    fold_state, unused = lax.scan(
        forward_one_step, fold_state, jnp.arange(extent // step_rows, dtype=jnp.int32)
    )
    row_top, row_total, row_acc = fold_state
    attn_heads = row_acc / row_total[:, :, None]
    log_total = row_top + jnp.log(row_total)
    attn_low = jnp.transpose(attn_heads, (1, 0, 2)).reshape(row_count, D).astype(jnp.bfloat16)
    branch_attn = jnp.dot(attn_low, out_weight, preferred_element_type=jnp.float32).astype(
        jnp.bfloat16
    )
    hidden_pre = jnp.dot(
        mlp_norm_low, up_weight, preferred_element_type=jnp.float32
    ) + up_bias.astype(jnp.float32)
    hidden, gelu_pull = jax.vjp(gelu_exact, hidden_pre)
    gate_half = hidden[:, :HALF]
    conv_norm, conv_pull = jax.vjp(
        norm_rows,
        hidden[:, HALF:],
        gate_norm_gain.astype(jnp.float32),
        gate_norm_bias.astype(jnp.float32),
    )
    conv_in = conv_norm.astype(jnp.bfloat16)
    half_width = KERNEL // 2
    conv_wide = extended(conv_in, (("tm", 0),), half_width)
    wide_frame, wide_item, wide_place = frame_info(
        stream_lengths, offset - half_width, row_count + 2 * half_width
    )
    kernel_rows = conv_kernel.astype(jnp.float32)
    conv_out = conv_bias.astype(jnp.float32) + jnp.zeros_like(gate_half)
    for tap_index in range(KERNEL):
        same_item = (wide_item[tap_index : tap_index + row_count] == item_of)[:, None]
        conv_out = (
            conv_out
            + jnp.where(
                same_item, conv_wide[tap_index : tap_index + row_count].astype(jnp.float32), 0.0
            )
            * kernel_rows[tap_index]
        )
    gated_low = (gate_half * conv_out).astype(jnp.bfloat16)
    branch_mlp = (
        jnp.dot(gated_low, down_weight, preferred_element_type=jnp.float32)
        + down_bias.astype(jnp.float32)
    ).astype(jnp.bfloat16)
    joined = jnp.concatenate([branch_attn, branch_mlp], axis=1)
    result = (
        inputs
        + jnp.dot(joined, merge_weight, preferred_element_type=jnp.float32)
        + merge_bias.astype(jnp.float32)
    )
    out_rows = result.astype(jnp.bfloat16)[None]
    grad_low = cotangent[0]
    grad_rows = grad_low.astype(jnp.float32)
    grad_merge_bias = jnp.sum(grad_rows, axis=0)
    grad_merge_weight = jnp.einsum(
        "tc,td->cd", joined, grad_low, preferred_element_type=jnp.float32
    )
    grad_joined = jnp.einsum(
        "td,cd->tc", grad_low, merge_weight, preferred_element_type=jnp.float32
    )
    grad_attn_branch = grad_joined[:, :D].astype(jnp.bfloat16)
    grad_mlp_branch = grad_joined[:, D:].astype(jnp.bfloat16)
    grad_down_weight = jnp.einsum(
        "tc,td->cd", gated_low, grad_mlp_branch, preferred_element_type=jnp.float32
    )
    grad_down_bias = jnp.sum(grad_mlp_branch.astype(jnp.float32), axis=0)
    grad_gated = jnp.einsum(
        "td,cd->tc", grad_mlp_branch, down_weight, preferred_element_type=jnp.float32
    )
    grad_gate_half = grad_gated * conv_out
    grad_conv_out = (grad_gated * gate_half).astype(jnp.bfloat16)
    grad_conv_rows = grad_conv_out.astype(jnp.float32)
    grad_conv_bias = jnp.sum(grad_conv_rows, axis=0)
    grad_wide = extended(grad_conv_out, (("tm", 0),), half_width)
    kernel_list = []
    grad_conv_in = jnp.zeros_like(grad_conv_rows)
    for tap_index in range(KERNEL):
        same_item = (wide_item[tap_index : tap_index + row_count] == item_of)[:, None]
        kernel_list.append(
            jnp.sum(
                jnp.where(
                    same_item, conv_wide[tap_index : tap_index + row_count].astype(jnp.float32), 0.0
                )
                * grad_conv_rows,
                axis=0,
            )
        )
        back_start = 2 * half_width - tap_index
        back_item = (wide_item[back_start : back_start + row_count] == item_of)[:, None]
        grad_conv_in = (
            grad_conv_in
            + jnp.where(
                back_item, grad_wide[back_start : back_start + row_count].astype(jnp.float32), 0.0
            )
            * kernel_rows[tap_index]
        )
    grad_conv_kernel = jnp.stack(kernel_list)
    grad_second, grad_gate_norm_gain, grad_gate_norm_bias = conv_pull(grad_conv_in)
    (grad_pre_rows,) = gelu_pull(jnp.concatenate([grad_gate_half, grad_second], axis=1))
    grad_pre = grad_pre_rows.astype(jnp.bfloat16)
    grad_up_bias = jnp.sum(grad_pre.astype(jnp.float32), axis=0)
    grad_up_weight = jnp.einsum(
        "tc,tf->cf", mlp_norm_low, grad_pre, preferred_element_type=jnp.float32
    )
    grad_mlp_norm = jnp.einsum("tf,cf->tc", grad_pre, up_weight, preferred_element_type=jnp.float32)
    grad_out_weight = jnp.einsum(
        "tc,td->cd", attn_low, grad_attn_branch, preferred_element_type=jnp.float32
    )
    grad_attn_low = jnp.einsum(
        "td,cd->tc", grad_attn_branch, out_weight, preferred_element_type=jnp.float32
    ).astype(jnp.bfloat16)
    grad_out_heads = grad_attn_low.reshape(row_count, HEADS, HEAD)
    delta_rows = jnp.sum(
        jnp.transpose(grad_out_heads.astype(jnp.float32), (1, 0, 2)) * attn_heads, axis=2
    )
    total_frames = row_count * cycle_size
    back_start_state = (
        jnp.zeros((row_count, HEADS, HEAD), jnp.float32),
        jnp.zeros((row_count, HEADS, D), jnp.float32),
        jnp.zeros((total_frames, D), jnp.float32),
        jnp.zeros((total_frames, D), jnp.float32),
    )
    back_key_piece = lax.all_gather(key_rows, "tm", axis=0, tiled=True)
    back_value_piece = lax.all_gather(value_rows, "tm", axis=0, tiled=True)
    extent = back_key_piece.shape[0]
    back_step_rows = step_size(extent)

    def back_one_step(inner_state, step_index):
        grad_content, grad_rel = inner_state
        key_block = lax.dynamic_slice_in_dim(
            back_key_piece, step_index * back_step_rows, back_step_rows, 0
        )
        value_block = lax.dynamic_slice_in_dim(
            back_value_piece, step_index * back_step_rows, back_step_rows, 0
        )
        prob_low, grad_raw, k_rel = block_grads(
            content_heads,
            q_rel,
            item_of,
            frame_index,
            grad_out_heads,
            log_total,
            delta_rows,
            key_block,
            value_block,
            step_index * back_step_rows,
            stream_lengths,
        )
        grad_content = grad_content + jnp.einsum(
            "hqk,khe->qhe",
            grad_raw,
            key_block.reshape(back_step_rows, HEADS, HEAD),
            preferred_element_type=jnp.float32,
        )
        grad_rel = grad_rel + jnp.einsum(
            "hqk,kc->qhc", grad_raw, k_rel, preferred_element_type=jnp.float32
        )
        key_part = jnp.einsum(
            "hqk,qhe->khe", grad_raw, content_heads, preferred_element_type=jnp.float32
        ).reshape(back_step_rows, D)
        value_part = jnp.einsum(
            "hqk,qhe->khe", prob_low, grad_out_heads, preferred_element_type=jnp.float32
        ).reshape(back_step_rows, D)
        return ((grad_content, grad_rel), (key_part, value_part))

    inner_state, block_parts = lax.scan(
        back_one_step,
        (back_start_state[0], back_start_state[1]),
        jnp.arange(extent // back_step_rows, dtype=jnp.int32),
    )
    key_all = block_parts[0].reshape(extent, D)
    value_all = block_parts[1].reshape(extent, D)
    grad_content, grad_rel, key_all, value_all = (
        inner_state[0],
        inner_state[1],
        key_all,
        value_all,
    )
    grad_keys, grad_values = (
        lax.psum_scatter(key_all, "tm", scatter_dimension=0, tiled=True),
        lax.psum_scatter(value_all, "tm", scatter_dimension=0, tiled=True),
    )
    half_size = D // 2
    rel_first = grad_rel[..., :half_size]
    rel_second = grad_rel[..., half_size:]
    sine_wide = sine_rows[:, None, :]
    cosine_wide = cosine_rows[:, None, :]
    grad_projected = jnp.concatenate(
        [
            rel_first * sine_wide - rel_second * cosine_wide,
            rel_first * cosine_wide + rel_second * sine_wide,
        ],
        axis=-1,
    ).astype(jnp.bfloat16)
    grad_pos_weight = jnp.einsum(
        "thc,the->che", grad_projected, position_heads, preferred_element_type=jnp.float32
    ).reshape(D, D)
    grad_q_position = jnp.einsum(
        "thc,che->the", grad_projected, pos_heads, preferred_element_type=jnp.float32
    )
    grad_content_bias = jnp.sum(grad_content, axis=0).reshape(D)
    grad_position_bias = jnp.sum(grad_q_position, axis=0).reshape(D)
    grad_query = (grad_content + grad_q_position).reshape(row_count, D).astype(jnp.bfloat16)
    grad_qkv = jnp.concatenate(
        [grad_query, grad_keys.astype(jnp.bfloat16), grad_values.astype(jnp.bfloat16)], axis=1
    )
    grad_qkv_weight = jnp.einsum(
        "tc,tf->cf", attn_norm_low, grad_qkv, preferred_element_type=jnp.float32
    )
    grad_attn_norm = jnp.einsum(
        "tf,cf->tc", grad_qkv, qkv_weight, preferred_element_type=jnp.float32
    )
    grad_from_attn, grad_ln_attn_gain, grad_ln_attn_bias = attn_pull(grad_attn_norm)
    grad_from_mlp, grad_ln_mlp_gain, grad_ln_mlp_bias = mlp_pull(grad_mlp_norm)
    grad_inputs = grad_rows + grad_from_attn + grad_from_mlp
    weight_grads = (
        grad_ln_attn_gain,
        grad_ln_attn_bias,
        grad_ln_mlp_gain,
        grad_ln_mlp_bias,
        grad_qkv_weight,
        grad_content_bias,
        grad_position_bias,
        grad_pos_weight,
        grad_out_weight,
        grad_up_weight,
        grad_up_bias,
        grad_gate_norm_gain,
        grad_gate_norm_bias,
        grad_conv_kernel,
        grad_conv_bias,
        grad_down_weight,
        grad_down_bias,
        grad_merge_weight,
        grad_merge_bias,
    )
    summed = lax.psum(
        (
            weight_grads[0],
            weight_grads[1],
            weight_grads[2],
            weight_grads[3],
            weight_grads[4],
            weight_grads[5],
            weight_grads[6],
            weight_grads[7],
            weight_grads[8],
            weight_grads[9],
            weight_grads[10],
            weight_grads[11],
            weight_grads[12],
            weight_grads[13],
            weight_grads[14],
            weight_grads[15],
            weight_grads[16],
            weight_grads[17],
            weight_grads[18],
        ),
        "tm",
    )
    shares = (
        lax.psum_scatter(
            summed[0].astype(jnp.bfloat16), "stream", scatter_dimension=0, tiled=True
        ).astype(jnp.float32),
        lax.psum_scatter(
            summed[1].astype(jnp.bfloat16), "stream", scatter_dimension=0, tiled=True
        ).astype(jnp.float32),
        lax.psum_scatter(
            summed[2].astype(jnp.bfloat16), "stream", scatter_dimension=0, tiled=True
        ).astype(jnp.float32),
        lax.psum_scatter(
            summed[3].astype(jnp.bfloat16), "stream", scatter_dimension=0, tiled=True
        ).astype(jnp.float32),
        lax.psum_scatter(
            summed[4].astype(jnp.bfloat16), "stream", scatter_dimension=0, tiled=True
        ).astype(jnp.float32),
        lax.psum_scatter(
            summed[5].astype(jnp.bfloat16), "stream", scatter_dimension=0, tiled=True
        ).astype(jnp.float32),
        lax.psum_scatter(
            summed[6].astype(jnp.bfloat16), "stream", scatter_dimension=0, tiled=True
        ).astype(jnp.float32),
        lax.psum_scatter(
            summed[7].astype(jnp.bfloat16), "stream", scatter_dimension=0, tiled=True
        ).astype(jnp.float32),
        lax.psum_scatter(
            summed[8].astype(jnp.bfloat16), "stream", scatter_dimension=0, tiled=True
        ).astype(jnp.float32),
        lax.psum_scatter(
            summed[9].astype(jnp.bfloat16), "stream", scatter_dimension=0, tiled=True
        ).astype(jnp.float32),
        lax.psum_scatter(
            summed[10].astype(jnp.bfloat16), "stream", scatter_dimension=0, tiled=True
        ).astype(jnp.float32),
        lax.psum_scatter(
            summed[11].astype(jnp.bfloat16), "stream", scatter_dimension=0, tiled=True
        ).astype(jnp.float32),
        lax.psum_scatter(
            summed[12].astype(jnp.bfloat16), "stream", scatter_dimension=0, tiled=True
        ).astype(jnp.float32),
        lax.psum_scatter(
            summed[13].astype(jnp.bfloat16), "stream", scatter_dimension=1, tiled=True
        ).astype(jnp.float32),
        lax.psum_scatter(
            summed[14].astype(jnp.bfloat16), "stream", scatter_dimension=0, tiled=True
        ).astype(jnp.float32),
        lax.psum_scatter(
            summed[15].astype(jnp.bfloat16), "stream", scatter_dimension=0, tiled=True
        ).astype(jnp.float32),
        lax.psum_scatter(
            summed[16].astype(jnp.bfloat16), "stream", scatter_dimension=0, tiled=True
        ).astype(jnp.float32),
        lax.psum_scatter(
            summed[17].astype(jnp.bfloat16), "stream", scatter_dimension=0, tiled=True
        ).astype(jnp.float32),
        lax.psum_scatter(
            summed[18].astype(jnp.bfloat16), "stream", scatter_dimension=0, tiled=True
        ).astype(jnp.float32),
    )
    return (out_rows, grad_inputs[None]) + tuple(shares)


LANES = 128
LOW = LANES // 2
BLOCK = 128
TALL = 256
WINDOW = 64
MARGIN = 16
BOUNDS = 16
MEGA = 1024 * 1024
F32 = jnp.float32
BF16 = jnp.bfloat16


def dot_nn(left, right):
    return jnp.dot(left, right, preferred_element_type=F32)


def dot_nt(left, right):
    return lax.dot_general(left, right, (((1,), (1,)), ((), ())), preferred_element_type=F32)


def dot_tn(left, right):
    return lax.dot_general(left, right, (((0,), (0,)), ((), ())), preferred_element_type=F32)


def rows_of(index, size, base=0):
    return pl.ds(pl.multiple_of(index * size, size) + base, size)


def line_of(ref):
    return ref[...].astype(F32).reshape(1, ref.shape[0])


def fold_rows(values):
    return jnp.sum(values.reshape(values.shape[0] // 8, 8, values.shape[1]), axis=0)


def one_row(values):
    return jnp.sum(values, axis=0, keepdims=True)


def turn(values):
    return pltpu.roll(values, LOW, 1)


def low_lanes(rows):
    return lax.broadcasted_iota(jnp.int32, (rows, LANES), 1) < LOW


def centre_rows(inputs):
    mean = jnp.mean(inputs, axis=-1, keepdims=True)
    centred = inputs - mean
    spread = jnp.mean(centred * centred, axis=-1, keepdims=True)
    return centred * lax.rsqrt(spread + EPS)


def gelu_parts(values):
    phi = 0.5 + 0.5 * lax.erf(values * math.sqrt(0.5))
    bell = jnp.exp(values * values * -0.5)
    return values * phi, phi + values * bell * (1.0 / math.sqrt(2.0 * math.pi))


class Part:
    def __init__(self, shape=None, pairs=None, refs=1, late=False):
        self.shape, self.pairs, self.refs, self.late = shape, pairs, refs, late

    def buffer(self, operand):
        return self.shape or operand.shape

    def copies(self, refs, buffer):
        return self.pairs(refs, buffer) if self.pairs else [(refs[0], buffer)]


def blocks_part(late=False):
    def pairs(refs, buffer):
        place = lax.axis_index("tm")
        return [
            (ref, buffer.at[rows_of(lax.bitwise_xor(jnp.int32(apart), place), BLOCK)])
            for apart, ref in enumerate(refs)
        ]

    return Part((HEADS * BLOCK, D), pairs, HEADS, late)


def rows_part(first, size, late=False):
    return Part((size, D), lambda refs, buffer: [(refs[0].at[pl.ds(first, size)], buffer)], late=late)


class Fetch:
    def __init__(self, pairs, buffer, sems, first):
        self.buffer, self.begun = buffer, False
        self.pending = [
            pltpu.make_async_copy(source, target, sems.at[first + index])
            for index, (source, target) in enumerate(pairs)
        ]

    def begin(self):
        if not self.begun:
            for copy in self.pending:
                copy.start()
        self.begun = True

    def __call__(self):
        self.begin()
        for copy in self.pending:
            copy.wait()
        self.pending = []
        return self.buffer


def begin(*fetches):
    for fetch in fetches:
        fetch.begin()


class Send:
    def __init__(self, buffer, target, sems):
        self.buffer, self.target, self.sems, self.copies = buffer, target, sems, []

    def go(self, *index):
        source, target = (self.buffer.at[index], self.target.at[index]) if index else (self.buffer, self.target)
        copy = pltpu.make_async_copy(source, target, self.sems[len(self.copies)])
        copy.start()
        self.copies.append(copy)

    def finish(self):
        if not self.copies:
            self.go()


SPACES = {"v": pltpu.VMEM, "s": pltpu.SMEM, "k": pl.ANY}


def kernel_call(body, out_shapes, plan, scratch=(), megas=58, bounds=False, aliases=None):
    def call(*operands):
        in_specs, buffers, at = [], [], 0
        for item in plan:
            if isinstance(item, Part):
                in_specs += [pl.BlockSpec(memory_space=pl.ANY)] * item.refs
                buffers.append(pltpu.VMEM(item.buffer(operands[at]), operands[at].dtype))
                at += item.refs
            else:
                in_specs.append(pl.BlockSpec(memory_space=SPACES[item]))
                at += 1
        sent = [out for out in out_shapes if len(out) > 2]
        buffers += [pltpu.VMEM(out[3] if len(out) > 3 else out[0], out[1]) for out in sent]
        sem_count = 64
        extra = [pltpu.SMEM((BOUNDS,), jnp.int32)] if bounds else []

        def outer(*refs):
            inputs, rest = refs[: len(in_specs)], refs[len(in_specs) :]
            outputs, rest = rest[: len(out_shapes)], rest[len(out_shapes) :]
            held, rest = list(rest[: len(buffers)]), rest[len(buffers) :]
            sems, rest = rest[0], rest[1:]
            given, at, used = [], 0, 0
            for item in plan:
                if isinstance(item, Part):
                    buffer = held.pop(0)
                    pairs = item.copies(inputs[at : at + item.refs], buffer)
                    given.append(Fetch(pairs, buffer, sems, used))
                    if not item.late:
                        given[-1].begin()
                    used += len(pairs)
                    at += item.refs
                else:
                    given.append(inputs[at])
                    at += 1
            results = []
            for out, ref in zip(out_shapes, outputs):
                if len(out) > 2:
                    target = out[4](ref) if len(out) > 3 else ref
                    results.append(Send(held.pop(0), target, [sems.at[used], sems.at[used + 1]]))
                    used += 2
                else:
                    results.append(ref)
            assert used <= sem_count
            body(*given, *results, *rest)
            for item in given:
                if isinstance(item, Fetch):
                    item()
            sends = [item for item in results if isinstance(item, Send)]
            for item in sends:
                item.finish()
            for item in sends:
                for copy in item.copies:
                    copy.wait()

        return pl.pallas_call(
            outer,
            out_shape=[jax.ShapeDtypeStruct(out[0], out[1]) for out in out_shapes],
            in_specs=in_specs,
            out_specs=[pl.BlockSpec(memory_space=pl.ANY if len(out) > 2 else pltpu.VMEM) for out in out_shapes],
            scratch_shapes=buffers
            + [pltpu.SemaphoreType.DMA((sem_count,))]
            + [pltpu.VMEM(shape, kind) for shape, kind in scratch]
            + extra,
            input_output_aliases=aliases or {},
            compiler_params=pltpu.CompilerParams(vmem_limit_bytes=megas * MEGA),
            cost_estimate=pl.CostEstimate(flops=0, bytes_accessed=0, transcendentals=0),
        )(*operands)

    return call


def fill_bounds(lengths_ref, bounds_s, total):
    bounds_s[0] = jnp.int32(0)
    end = jnp.int32(0)
    for item in range(ITEMS):
        end = end + lengths_ref[0, item]
        bounds_s[item + 1] = end
    for item in range(ITEMS + 1, BOUNDS):
        bounds_s[item] = jnp.int32(total)


def select_kernel(
    up_ref,
    up_bias_ref,
    gain_ref,
    bias_ref,
    conv_bias_ref,
    taps_ref,
    qkv_ref,
    pos_ref,
    content_ref,
    position_ref,
    up_out,
    table_out,
    qkv_out,
    pos_out,
    bias_out,
):
    place = lax.axis_index("tm")
    quarters = lax.axis_size("stream")
    share = HALF // (quarters * lax.axis_size("tm"))
    lane = lax.broadcasted_iota(jnp.int32, (1, 2 * LANES), 1)
    channel = jnp.where(lane < LANES + LOW, lane, lane - LOW)
    group = jnp.zeros_like(channel)
    for quarter in range(1, quarters):
        group = group + (channel >= quarter * share).astype(jnp.int32)
    source = group * (HALF // quarters) + share * place + channel - group * share
    chosen = (lax.broadcasted_iota(jnp.int32, (HALF, 2 * LANES), 0) == source).astype(F32).astype(BF16)
    gate = dot_nn(up_ref[:, :HALF], chosen)
    conv = dot_nn(up_ref[:, HALF:], chosen)
    up_out[:, :LANES] = gate[:, :LANES].astype(BF16)
    up_out[:, LANES : 2 * LANES] = jnp.where(low_lanes(D), gate[:, LANES:], conv[:, LANES:]).astype(BF16)
    up_out[:, 2 * LANES :] = conv[:, :LANES].astype(BF16)
    up_bias = line_of(up_bias_ref)
    lines = jnp.concatenate(
        [
            up_bias[:, :HALF],
            up_bias[:, HALF:],
            line_of(gain_ref),
            line_of(bias_ref),
            line_of(conv_bias_ref),
            jnp.zeros((3, HALF), F32),
        ],
        axis=0,
    )
    lines = dot_nn(lines.astype(BF16), chosen)
    taps = dot_nn(taps_ref[...], chosen)
    for part in range(2):
        lanes = slice(part * LANES, (part + 1) * LANES)
        table_out[part, :8] = lines[:, lanes]
        table_out[part, 8 : 8 + KERNEL] = taps[:, lanes]
        table_out[part, 8 + KERNEL :] = jnp.zeros((1, LANES), F32)

    odd = lax.rem(place, 2) == 1

    def head_lanes(ref, base):
        at = pl.ds(pl.multiple_of(lax.div(place, 2) * LANES + base, LANES), LANES)
        values = ref[:, at].astype(F32)
        values = jnp.where(odd, turn(values), values)
        return jnp.where(low_lanes(values.shape[0]), values, 0.0)

    for part in range(3):
        qkv_out[:, part * LANES : (part + 1) * LANES] = head_lanes(qkv_ref, part * D).astype(BF16)
    pos_out[...] = head_lanes(pos_ref, 0).astype(BF16)
    bias_out[...] = jnp.zeros((8, LANES), F32)
    for line, ref in enumerate((content_ref, position_ref)):
        values = line_of(ref)
        picked = values[:, :LANES]
        for tile in range(1, D // LANES):
            picked = jnp.where(
                lax.div(place, 2) == tile, values[:, tile * LANES : (tile + 1) * LANES], picked
            )
        picked = jnp.where(odd, turn(picked), picked)
        bias_out[line : line + 1] = jnp.where(low_lanes(1), picked, 0.0)


def angle_rows(coarse_ref, fine_ref, block, rows):
    half = D // 2
    base = coarse_ref[pl.ds(block, 1)]
    base_sine, base_cosine = base[:, :half], base[:, half:]
    sine, cosine = fine_ref[rows, :half], fine_ref[rows, half:]
    return base_sine * cosine + base_cosine * sine, base_cosine * cosine - base_sine * sine


def item_codes(bounds_s, index):
    code = jnp.zeros_like(index)
    for item in range(1, ITEMS + 1):
        code = code + (index >= bounds_s[item]).astype(jnp.int32)
    return jnp.where(code < ITEMS, code, ITEMS + index)


def attend_kernel(
    lengths_ref,
    x_ref,
    attn_gain_ref,
    attn_bias_ref,
    mlp_gain_ref,
    mlp_bias_ref,
    qkv_ref,
    pos_ref,
    bias_ref,
    coarse_ref,
    fine_ref,
    up_ref,
    up_bias_ref,
    n_attn_out,
    n_mlp_out,
    hat_out,
    q_position_out,
    query_out,
    key_out,
    value_out,
    prob_out,
    attn_out,
    share_out,
    stats_out,
    pre_s,
    bounds_s,
):
    frames = n_attn_out.buffer.shape[0]
    half = D // 2
    fill_bounds(lengths_ref, bounds_s, frames)
    attn_gain, attn_bias = line_of(attn_gain_ref), line_of(attn_bias_ref)
    mlp_gain, mlp_bias = line_of(mlp_gain_ref), line_of(mlp_bias_ref)
    content, position = bias_ref[0:1], bias_ref[1:2]
    x_ref = x_ref()
    begin(up_ref)

    @pl.loop(0, frames // TALL, unroll=2)
    def _(block):
        rows = rows_of(block, TALL)
        for part in range(TALL // 32):
            at = rows_of(block, TALL, part * 32)
            at = pl.ds(pl.multiple_of(block * TALL + part * 32, 32), 32)
            hat = centre_rows(x_ref[at].astype(F32))
            hat_out.buffer[at] = hat.astype(BF16)
            n_attn_out.buffer[at] = (hat * attn_gain + attn_bias).astype(BF16)
            n_mlp_out.buffer[at] = (hat * mlp_gain + mlp_bias).astype(BF16)
        parts = dot_nn(n_attn_out.buffer[rows], qkv_ref[...])
        query = parts[:, :LANES]
        query_out.buffer[rows, :LANES] = ((query + content).astype(BF16).astype(F32) * 0.125).astype(BF16)
        q_position = (query + position).astype(BF16)
        q_position_out.buffer[rows] = q_position
        key_out.buffer[rows, :LANES] = parts[:, LANES : 2 * LANES].astype(BF16)
        value_out.buffer[rows] = parts[:, 2 * LANES :].astype(BF16)
        projected = dot_nt(q_position, pos_ref[...])
        for part in range(TALL // 32):
            at = pl.ds(pl.multiple_of(block * TALL + part * 32, 32), 32)
            inner = part * 32 % BLOCK
            sine, cosine = angle_rows(
                coarse_ref, fine_ref, block * (TALL // BLOCK) + part * 32 // BLOCK, slice(inner, inner + 32)
            )
            first = projected[part * 32 : part * 32 + 32, :half]
            second = projected[part * 32 : part * 32 + 32, half:]
            query_out.buffer[at, LANES : LANES + half] = ((first * sine + second * cosine) * 0.125).astype(BF16)
            query_out.buffer[at, LANES + half :] = ((second * sine - first * cosine) * 0.125).astype(BF16)
            key_out.buffer[at, LANES : LANES + half] = cosine.astype(BF16)
            key_out.buffer[at, LANES + half :] = sine.astype(BF16)

    for out in (n_attn_out, n_mlp_out, hat_out, q_position_out, query_out, key_out, value_out):
        out.go()
    up_ref = up_ref()
    up_bias = line_of(up_bias_ref)[:, HALF:]
    lane = lax.broadcasted_iota(jnp.int32, (16, LANES), 1)

    @pl.loop(0, frames // BLOCK)
    def _(block):
        pre_s[...] = dot_nn(n_mlp_out.buffer[rows_of(block, BLOCK)], up_ref[...])
        for part in range(BLOCK // 16):
            pre = pre_s[part * 16 : part * 16 + 16] + up_bias
            hidden = pre * (0.5 + 0.5 * lax.erf(pre * math.sqrt(0.5)))
            mean = jnp.mean(hidden, axis=-1, keepdims=True)
            centred = hidden - mean
            rate = lax.rsqrt(jnp.mean(centred * centred, axis=-1, keepdims=True) + EPS)
            at = pl.ds(pl.multiple_of(block * BLOCK + part * 16, 16), 16)
            stats_out.buffer[at] = jnp.where(lane == 0, mean, rate)

    stats_out.go()
    key_code = item_codes(bounds_s, lax.broadcasted_iota(jnp.int32, (1, frames), 1))

    @pl.loop(0, frames // TALL, unroll=2)
    def _(block):
        rows = rows_of(block, TALL)
        raw = dot_nt(query_out.buffer[rows], key_out.buffer[...])
        for part in range(TALL // 32):
            start = block * TALL + part * 32
            at = pl.ds(pl.multiple_of(start, 32), 32)
            index = start + lax.broadcasted_iota(jnp.int32, (32, 1), 0)
            scaled = jnp.where(
                item_codes(bounds_s, index) == key_code, raw[part * 32 : part * 32 + 32], MASKED
            )
            weight = jnp.exp(scaled - jnp.max(scaled, axis=1, keepdims=True))
            prob_out.buffer[at] = weight.astype(BF16)
            share_out.buffer[at] = jnp.broadcast_to(1.0 / jnp.sum(weight, axis=1, keepdims=True), (32, LANES))
        attn_out.buffer[rows] = (
            dot_nn(prob_out.buffer[rows], value_out.buffer[...]) * share_out.buffer[rows]
        )


def fill_margins(wide_s, frames):
    edge = jnp.zeros((MARGIN, LANES), F32)
    wide_s[:MARGIN] = edge
    wide_s[MARGIN + frames : 2 * MARGIN + frames] = edge
    base = frames + 3 * MARGIN
    after = base + frames // 2
    low = low_lanes(MARGIN)
    wide_s[base - MARGIN : base] = jnp.where(low, 0.0, turn(wide_s[after - MARGIN : after]))
    wide_s[after : after + MARGIN] = jnp.where(low, turn(wide_s[base : base + MARGIN]), 0.0)


def item_span(bounds_s, frame):
    begin, end = bounds_s[0], bounds_s[BOUNDS - 1]
    for item in range(1, ITEMS + 1):
        edge = bounds_s[item]
        begin = jnp.where(frame >= edge, edge, begin)
    for item in range(ITEMS, 0, -1):
        edge = bounds_s[item]
        end = jnp.where(frame < edge, edge, end)
    return begin, end


def is_whole(bounds_s, start):
    begin, end = item_span(bounds_s, start)
    reach = KERNEL // 2
    low = (begin == 0) | (begin <= start - reach)
    high = (end == bounds_s[BOUNDS - 1]) | (end >= start + WINDOW + reach)
    return low & high & (end >= start + WINDOW)


def tap_limits(bounds_s, start):
    frame = start + lax.broadcasted_iota(jnp.int32, (WINDOW, LANES), 0)
    begin, end = item_span(bounds_s, frame)
    return begin - frame, end - frame


def grouped(values):
    return values.reshape(WINDOW // 8, 8, LANES)


def triple_places(step, frames):
    half = frames // 2
    return (
        pl.multiple_of(step * WINDOW, 2 * MARGIN),
        pl.multiple_of(step * WINDOW + half, 2 * MARGIN),
        pl.multiple_of(step * WINDOW + frames + 2 * MARGIN, 2 * MARGIN),
    )


def over_windows(bounds_s, frames, body):
    half = frames // 2

    @pl.loop(0, half // WINDOW)
    def _(step):
        start = step * WINDOW
        whole = is_whole(bounds_s, start) & is_whole(bounds_s, start + half)

        @pl.when(whole)
        def _():
            body(step, None)

        @pl.when(jnp.logical_not(whole))
        def _():
            first, second = tap_limits(bounds_s, start), tap_limits(bounds_s, start + half)
            low = low_lanes(WINDOW)
            rest = [jnp.where(low, one, other) for one, other in zip(first, second)]
            body(step, (first, second, rest))


def tap_view(window_ref, tap, limits):
    view = window_ref[tap + 1 : tap + 1 + WINDOW]
    if limits is not None:
        shift = tap - KERNEL // 2
        view = jnp.where((limits[0] <= shift) & (limits[1] > shift), view, 0.0)
    return grouped(view)


def mlp_first_kernel(
    lengths_ref,
    n_ref,
    up_ref,
    table_ref,
    stats_ref,
    cot_ref,
    merge_ref,
    down_ref,
    attn_ref,
    mixed_out,
    gate_pre_out,
    grad_out,
    rate_out,
    hat_out,
    early_out,
    vectors_out,
    lines_out,
    hat_s,
    slope_s,
    gate_s,
    hidden_s,
    gate_slope_s,
    conv_s,
    grad_s,
    out_s,
    back_s,
    branch_s,
    mix_s,
    taps_s,
    turn_s,
    tap_sum_s,
    columns_s,
    forward_s,
    backward_s,
    bounds_s,
):
    frames = mix_s.shape[0]
    half = frames // 2
    blocks = frames // BLOCK
    quarters, early_rows, _ = early_out.buffer.shape
    share = early_rows // 8
    channels = quarters * share
    fill_bounds(lengths_ref, bounds_s, frames)
    for part in range(2):
        for tap in range(KERNEL):
            line = jnp.broadcast_to(table_ref[part, 8 + tap : 9 + tap], (8, LANES))
            taps_s[part, tap] = line
            turn_s[part, KERNEL - 1 - tap] = line
    tap_sum_s[...] = jnp.zeros(tap_sum_s.shape, F32)
    main, rest = table_ref[0, :8], table_ref[1, :8]
    mixed_bias = jnp.where(low_lanes(1), rest[0:1], rest[1:2])
    low = low_lanes(64)
    gate_pre_ref = gate_pre_out.buffer
    n_ref = n_ref()
    stats_ref = stats_ref()
    begin(cot_ref, merge_ref, down_ref, attn_ref)

    def stat_rows(rows):
        stats = stats_ref[rows]
        return stats[:, 0:1], stats[:, 1:2]

    def chunk(start, base=0):
        return pl.ds(pl.multiple_of(start, 64) + base, 64)

    def conv_part(hidden, mean, rate, lines, rows, to_rows):
        hat = (hidden - mean) * rate
        hat_s[rows] = hat
        hat_out.buffer[rows] = hat.astype(BF16)
        conv_s[to_rows] = (hat * lines[2:3] + lines[3:4]).astype(BF16).astype(F32)

    @pl.loop(0, half // TALL)
    def _(block):
        pre = [dot_nn(n_ref[rows_of(block, TALL, base)], up_ref[...]) for base in (0, half)]
        for part in range(TALL // 64):
            inner = slice(part * 64, part * 64 + 64)
            start = block * TALL + part * 64
            mixed = []
            for values, base in zip(pre, (0, half)):
                rows = chunk(start, base)
                gate, gate_slope = gelu_parts(values[inner, :LANES] + main[0:1])
                hidden_s[rows] = gate
                gate_slope_s[rows] = gate_slope
                hidden, slope = gelu_parts(values[inner, 2 * LANES :] + main[1:2])
                mean, rate = stat_rows(rows)
                slope_s[rows] = slope * rate
                conv_part(hidden, mean, rate, main, rows, chunk(start, base + MARGIN))
                mixed.append((*gelu_parts(values[inner, LANES : 2 * LANES] + mixed_bias), mean, rate))
            (low_hidden, low_slope, low_mean, low_rate), (high_hidden, high_slope, high_mean, high_rate) = mixed
            rows = chunk(start, frames)
            hidden_s[rows] = jnp.where(low, low_hidden, turn(high_hidden))
            gate_slope_s[rows] = jnp.where(low, low_slope, turn(high_slope))
            rate = jnp.where(low, low_rate, high_rate)
            slope_s[rows] = jnp.where(low, turn(low_slope), high_slope) * rate
            conv_part(
                jnp.where(low, turn(low_hidden), high_hidden),
                jnp.where(low, low_mean, high_mean),
                rate,
                rest,
                rows,
                chunk(start, frames + 3 * MARGIN),
            )

    hat_out.go()
    fill_margins(conv_s, frames)
    tall = WINDOW + 2 * MARGIN
    outs = (0, half, frames)

    def convolve(step, limits):
        for index, base in enumerate(triple_places(step, frames)):
            forward_s[index] = conv_s[pl.ds(base, tall)]
        for index in range(3):
            own = None if limits is None else limits[index]
            total = jnp.zeros((WINDOW // 8, 8, LANES), F32)
            for tap in range(KERNEL):
                total = total + tap_view(forward_s.at[index], tap, own) * taps_s[index // 2, tap][None]
            lines = rest if index == 2 else main
            out_s[rows_of(step, WINDOW, outs[index])] = total.reshape(WINDOW, LANES) + lines[4:5]

    over_windows(bounds_s, frames, convolve)
    cot_ref = cot_ref()
    merge_ref = merge_ref()
    down_ref = down_ref()
    attn_ref = attn_ref()
    down_ref[channels:] = jnp.zeros((2 * LANES - channels, D), BF16)
    zero = jnp.zeros((8, LANES), F32)

    def branch_part(grad_gated, rows, to_rows, sums):
        up_sum, conv_sum = sums
        gate, conv = hidden_s[rows], out_s[rows]
        gate_pre = (grad_gated * conv * gate_slope_s[rows]).astype(BF16)
        gate_pre_ref[rows] = gate_pre
        grad_conv = (grad_gated * gate).astype(BF16).astype(F32)
        grad_s[to_rows] = grad_conv
        gate_pre = gate_pre.astype(F32)
        return gate * conv, gate_pre, (up_sum + fold_rows(gate_pre), conv_sum + fold_rows(grad_conv))

    def branch_step(block, sums):
        main_sums, rest_sums = sums
        grads = []
        for base in (0, half):
            rows = rows_of(block, TALL, base)
            branch = dot_nt(cot_ref[rows], merge_ref[...]).astype(BF16)
            branch_s[rows] = branch
            grads.append(dot_nt(branch, down_ref[...]))
        for part in range(TALL // 64):
            inner = slice(part * 64, part * 64 + 64)
            start = block * TALL + part * 64
            for values, base in zip(grads, (0, half)):
                rows = chunk(start, base)
                gated, gate_pre, main_sums = branch_part(
                    values[inner, :LANES], rows, chunk(start, base + MARGIN), main_sums
                )
                mix_s[rows, :LANES] = gated.astype(BF16)
                gate_s[rows, :LANES] = gate_pre.astype(BF16)
            grad = jnp.where(low, grads[0][inner, LANES:], turn(grads[1][inner, LANES:]))
            gated, gate_pre, rest_sums = branch_part(
                grad, chunk(start, frames), chunk(start, frames + 3 * MARGIN), rest_sums
            )
            low_rows, high_rows = chunk(start), chunk(start, half)
            gate_s[low_rows, LANES:] = gate_pre.astype(BF16)
            gate_s[high_rows, LANES:] = turn(gate_pre).astype(BF16)
            mix_s[low_rows, LANES:] = jnp.where(low, gated, turn(attn_ref[low_rows])).astype(BF16)
            mix_s[high_rows, LANES:] = jnp.where(low, turn(gated), turn(attn_ref[high_rows])).astype(BF16)
        return main_sums, rest_sums

    (main_up, main_conv), (rest_up, rest_conv) = lax.fori_loop(
        0, half // TALL, branch_step, ((zero, zero), (zero, zero))
    )
    gate_pre_out.go()
    fill_margins(grad_s, frames)
    ones = jnp.ones((16, frames), BF16)
    lines_out[0:1] = dot_nn(ones, branch_s[...])[0:1]
    lines_out[1:2] = dot_nn(ones, cot_ref[...])[0:1]
    lines_out[2:8] = jnp.zeros((6, D), F32)
    grad_down = dot_tn(mix_s[...], branch_s[...])
    grad_gate = dot_tn(gate_s[...], n_ref[...])
    for quarter in range(quarters):
        for tile in range(4):
            early_out.buffer[quarter, tile * share : (tile + 1) * share] = grad_down[
                quarter * share : (quarter + 1) * share, tile * LANES : (tile + 1) * LANES
            ].astype(BF16)
        early_out.buffer[quarter, 4 * share :] = grad_gate[
            :channels, quarter * LANES : (quarter + 1) * LANES
        ].astype(BF16)
    early_out.go()
    for block in range(blocks):
        mixed_out.buffer[block, :BLOCK] = mix_s[block * BLOCK : (block + 1) * BLOCK]
    mixed_out.go(slice(None), pl.ds(0, BLOCK))

    def differentiate(step, limits):
        for index, base in enumerate(triple_places(step, frames)):
            forward_s[index] = conv_s[pl.ds(base, tall)]
            backward_s[index] = grad_s[pl.ds(base, tall)]
        for index in range(3):
            own = None if limits is None else limits[index]
            total = jnp.zeros((WINDOW // 8, 8, LANES), F32)
            centre = grouped(backward_s[index, MARGIN : MARGIN + WINDOW])
            for tap in range(KERNEL):
                total = total + tap_view(backward_s.at[index], tap, own) * turn_s[index // 2, tap][None]
                tap_sum_s[index // 2, tap] += jnp.sum(tap_view(forward_s.at[index], tap, own) * centre, axis=0)
            back_s[rows_of(step, WINDOW, outs[index])] = total.reshape(WINDOW, LANES)

    over_windows(bounds_s, frames, differentiate)
    lane = lax.broadcasted_iota(jnp.int32, (64, LANES), 1)

    def norm_part(rows, lines, sums):
        gain_sum, bias_sum = sums
        back, hat, slope = back_s[rows], hat_s[rows], slope_s[rows]
        grad = back * lines[2:3]
        grad_out.buffer[rows] = (grad * slope).astype(BF16)
        rate_out.buffer[rows] = slope.astype(BF16)
        along = back * hat
        return grad, along * lines[2:3], (gain_sum + fold_rows(along), bias_sum + fold_rows(back))

    def norm_step(block, sums):
        main_sums, rest_sums = sums
        for part in range(TALL // 64):
            start = block * TALL + part * 64
            pairs = []
            for base in (0, half):
                plain, along, main_sums = norm_part(chunk(start, base), main, main_sums)
                pairs.append([plain, along])
            plain, along, rest_sums = norm_part(chunk(start, frames), rest, rest_sums)
            for item, values in enumerate((plain, along)):
                pairs[0][item] = pairs[0][item] + jnp.where(low, values, 0.0)
                pairs[1][item] = pairs[1][item] + jnp.where(low, 0.0, values)
            for (plain, along), base in zip(pairs, (0, half)):
                columns_s[chunk(start, base)] = jnp.where(
                    lane == 0,
                    jnp.sum(plain, axis=-1, keepdims=True),
                    jnp.where(lane == 1, jnp.sum(along, axis=-1, keepdims=True), 0.0),
                )
        return main_sums, rest_sums

    (main_gain, main_bias), (rest_gain, rest_bias) = lax.fori_loop(
        0, half // TALL, norm_step, ((zero, zero), (zero, zero))
    )
    grad_out.go()
    rate_out.go()
    totals = jnp.concatenate(
        [jnp.transpose(columns_s[block * BLOCK : (block + 1) * BLOCK])[:2] for block in range(blocks)], axis=0
    )
    high = totals.astype(BF16)
    low_part = (totals - high.astype(F32)).astype(BF16)
    for block in range(blocks):
        mixed_out.buffer[block, BLOCK:, :LANES] = high
        mixed_out.buffer[block, BLOCK:, LANES:] = low_part
    mixed_out.go(slice(None), pl.ds(BLOCK, 2 * blocks))

    def vectors(part, lines):
        taps = jnp.sum(tap_sum_s[part], axis=1)[:KERNEL]
        stacked = jnp.concatenate([taps] + [one_row(line) for line in lines], axis=0)
        if part:
            stacked = stacked + turn(stacked)
        return jnp.transpose(
            jnp.concatenate([stacked, jnp.zeros((LANES - stacked.shape[0], LANES), F32)], axis=0)
        )

    vectors_out[:LANES] = vectors(0, (main_conv, main_gain, main_bias, main_up))
    vectors_out[LANES:] = vectors(1, (rest_conv, rest_gain, rest_bias, rest_up))[: channels - LANES]


def attend_back_kernel(
    cot_ref,
    merge_ref,
    head_ref,
    share_ref,
    value_ref,
    attn_ref,
    prob_ref,
    key_ref,
    coarse_ref,
    fine_ref,
    pos_ref,
    query_ref,
    n_ref,
    q_position_ref,
    qkv_ref,
    hat_ref,
    gain_ref,
    early_ref,
    branch_out,
    total_out,
    pack_0,
    pack_1,
    pack_2,
    pack_3,
    lines_out,
    grad_s,
    raw_s,
    projected_s,
    parts_s,
    grads_s,
):
    place = lax.axis_index("tm")
    frames = raw_s.shape[0]
    blocks = frames // BLOCK
    half = D // 2
    zero = jnp.zeros((8, LANES), F32)
    cot_ref, merge_ref, head_ref, share_ref = cot_ref(), merge_ref(), head_ref(), share_ref()
    head_ref[HEAD:] = jnp.zeros((LANES - HEAD, D), BF16)
    begin(value_ref, attn_ref, prob_ref, key_ref, pos_ref)

    @pl.loop(0, frames // TALL, unroll=2)
    def _(block):
        rows = rows_of(block, TALL)
        branch = dot_nt(cot_ref[rows], merge_ref[...]).astype(BF16)
        branch_out.buffer[rows] = branch
        grad_s[rows] = (dot_nt(branch, head_ref[...]) * share_ref[rows]).astype(BF16)

    branch_out.go()
    value_ref, attn_ref, prob_ref = value_ref(), attn_ref(), prob_ref()
    key_ref, pos_ref = key_ref(), pos_ref()
    begin(query_ref, n_ref, q_position_ref, qkv_ref, hat_ref, early_ref)

    def score_step(block, sums):
        content_sum, position_sum = sums
        rows = rows_of(block, TALL)
        grad = grad_s[rows]
        score = dot_nt(grad, value_ref[...])
        for part in range(TALL // 32):
            at = pl.ds(pl.multiple_of(block * TALL + part * 32, 32), 32)
            inner = slice(part * 32, part * 32 + 32)
            delta = jnp.sum(grad[inner].astype(F32) * attn_ref[at], axis=1, keepdims=True)
            raw_s[at] = (prob_ref[at].astype(F32) * (score[inner] - delta)).astype(BF16)
        query = dot_nn(raw_s[rows], key_ref[...]) * 0.125
        for part in range(TALL // 32):
            at = pl.ds(pl.multiple_of(block * TALL + part * 32, 32), 32)
            inner = part * 32 % BLOCK
            sine, cosine = angle_rows(
                coarse_ref, fine_ref, block * (TALL // BLOCK) + part * 32 // BLOCK, slice(inner, inner + 32)
            )
            inner = slice(part * 32, part * 32 + 32)
            first, second = query[inner, LANES : LANES + half], query[inner, LANES + half :]
            projected_s[at, :half] = (first * sine - second * cosine).astype(BF16)
            projected_s[at, half:] = (first * cosine + second * sine).astype(BF16)
        position = dot_nn(projected_s[rows], pos_ref[...])
        content = query[:, :LANES]
        parts_s[rows, :LANES] = (content + position).astype(BF16)
        return content_sum + fold_rows(content), position_sum + fold_rows(position)

    content_sum, position_sum = lax.fori_loop(0, frames // TALL, score_step, (zero, zero), unroll=2)
    query_ref, n_ref, q_position_ref = query_ref(), n_ref(), q_position_ref()
    qkv_ref, hat_ref = qkv_ref(), hat_ref()
    grad_key = dot_tn(query_ref[...], raw_s[...])
    grad_value = dot_tn(grad_s[...], prob_ref[...])
    for block in range(blocks):
        at = slice(block * BLOCK, (block + 1) * BLOCK)
        parts_s[at, LANES : 2 * LANES] = jnp.transpose(grad_key[:, at]).astype(BF16)
        parts_s[at, 2 * LANES :] = jnp.transpose(grad_value[:, at]).astype(BF16)
    grads_s[:HEAD] = dot_tn(parts_s[:, :LANES], n_ref[...])[:HEAD]
    grads_s[HEAD : 2 * HEAD] = dot_nn(grad_key.astype(BF16), n_ref[...])[:HEAD]
    grads_s[2 * HEAD : 3 * HEAD] = dot_nn(grad_value.astype(BF16), n_ref[...])[:HEAD]
    grads_s[3 * HEAD :] = dot_tn(q_position_ref[...], projected_s[...])[:HEAD]
    stream = lax.axis_index("stream")
    early_ref = early_ref()
    for apart, pack_out in enumerate((pack_0, pack_1, pack_2, pack_3)):
        quarter = lax.bitwise_xor(stream, jnp.int32(apart))
        lanes = pl.ds(pl.multiple_of(quarter * LANES, LANES), LANES)
        pack_out.buffer[: 4 * HEAD] = grads_s[:, lanes].astype(BF16)
        pack_out.buffer[4 * HEAD :] = early_ref[quarter]
        pack_out.go()
    gain = line_of(gain_ref)
    wide_zero = jnp.zeros((8, D), F32)

    def norm_step(block, sums):
        gain_sum, bias_sum = sums
        grad = dot_nt(parts_s[rows_of(block, TALL)], qkv_ref[...])
        for part in range(TALL // 32):
            at = pl.ds(pl.multiple_of(block * TALL + part * 32, 32), 32)
            own = grad[part * 32 : part * 32 + 32]
            total_out.buffer[at] = (own * gain).astype(BF16)
            gain_sum = gain_sum + fold_rows(own * hat_ref[at].astype(F32))
            bias_sum = bias_sum + fold_rows(own)
        return gain_sum, bias_sum

    gain_sum, bias_sum = lax.fori_loop(0, frames // TALL, norm_step, (wide_zero, wide_zero), unroll=2)
    lane = lax.broadcasted_iota(jnp.int32, (1, LANES), 1)

    def own_lanes(sums):
        line = one_row(sums)
        line = line + turn(line)
        tiles = [
            jnp.where(lax.div(tile * LANES + lane, HEAD) == place, line, 0.0) for tile in range(D // LANES)
        ]
        return jnp.concatenate(tiles, axis=1)

    lines_out[...] = jnp.concatenate(
        [
            one_row(gain_sum),
            one_row(bias_sum),
            own_lanes(content_sum),
            own_lanes(position_sum),
            jnp.zeros((4, D), F32),
        ],
        axis=0,
    )


def mlp_second_kernel(
    mixed_ref,
    gate_pre_ref,
    grad_ref,
    rate_ref,
    hat_ref,
    up_ref,
    norm_hat_ref,
    gain_ref,
    other_ref,
    n_ref,
    vectors_ref,
    first_lines_ref,
    head_lines_ref,
    total_out,
    pack_0,
    pack_1,
    pack_2,
    pack_3,
    pre_s,
    columns_s,
    grad_up_s,
    lines_s,
    up_columns_s,
):
    packs = (pack_0, pack_1, pack_2, pack_3)
    stream = lax.axis_index("stream")
    place = lax.axis_index("tm")
    frames = pre_s.shape[0]
    half = frames // 2
    blocks = frames // BLOCK
    quarters = len(packs)
    channels = vectors_ref.shape[0]
    share = channels // quarters
    totals = jnp.zeros((2 * blocks, LANES), F32)
    mixed_ref = mixed_ref()
    for source in range(mixed_ref.shape[0]):
        both = mixed_ref[source].astype(F32)
        totals = totals + (both[:, :LANES] + both[:, LANES:])
    totals = totals * (1.0 / HALF)
    columns = jnp.transpose(jnp.concatenate([totals, jnp.zeros((LANES - 2 * blocks, LANES), F32)], axis=0))
    lane = lax.broadcasted_iota(jnp.int32, (BLOCK, LANES), 1)
    for block in range(blocks):
        columns_s[block * BLOCK : (block + 1) * BLOCK] = jnp.where(
            lane == 0, columns[:, 2 * block : 2 * block + 1], columns[:, 2 * block + 1 : 2 * block + 2]
        )
    gate_pre_ref, grad_ref, rate_ref, hat_ref = gate_pre_ref(), grad_ref(), rate_ref(), hat_ref()
    begin(n_ref, up_ref, norm_hat_ref, other_ref)
    low = low_lanes(64)
    gain = line_of(gain_ref)

    def chunk(start, base=0):
        return pl.ds(pl.multiple_of(start, 64) + base, 64)

    def pre_part(rows, table, up_sum):
        plain, along = table
        hat, rate = hat_ref[rows].astype(F32), rate_ref[rows].astype(F32)
        pre = (grad_ref[rows].astype(F32) - rate * (plain + hat * along)).astype(BF16).astype(F32)
        return pre, up_sum + fold_rows(pre)

    def pre_step(block, sums):
        main_up, rest_up = sums
        for part in range(TALL // 64):
            start = block * TALL + part * 64
            tables = []
            for base in (0, half):
                rows = chunk(start, base)
                values = columns_s[rows]
                table = [values[:, item : item + 1] for item in range(2)]
                tables.append(table)
                pre, main_up = pre_part(rows, table, main_up)
                pre_s[rows, :LANES] = gate_pre_ref[rows]
                pre_s[rows, 2 * LANES :] = pre.astype(BF16)
            rows = chunk(start, frames)
            table = [jnp.where(low, one, other) for one, other in zip(*tables)]
            pre, rest_up = pre_part(rows, table, rest_up)
            gate_pre = gate_pre_ref[rows].astype(F32)
            pre_s[chunk(start), LANES : 2 * LANES] = jnp.where(low, gate_pre, turn(pre)).astype(BF16)
            pre_s[chunk(start, half), LANES : 2 * LANES] = jnp.where(low, turn(gate_pre), pre).astype(BF16)
        return main_up, rest_up

    zero = jnp.zeros((8, LANES), F32)
    main_up, rest_up = lax.fori_loop(0, half // TALL, pre_step, (zero, zero))
    n_ref, up_ref, norm_hat_ref, other_ref = n_ref(), up_ref(), norm_hat_ref(), other_ref()
    grad_up_s[...] = dot_tn(pre_s[:, LANES:], n_ref[...])
    wide_zero = jnp.zeros((8, D), F32)

    def norm_step(block, sums):
        gain_sum, bias_sum = sums
        rows = rows_of(block, BLOCK)
        grad = dot_nt(pre_s[rows], up_ref[...])
        total_out.buffer[block] = (grad * gain + other_ref[rows].astype(F32)).astype(BF16)
        return gain_sum + fold_rows(grad * norm_hat_ref[rows].astype(F32)), bias_sum + fold_rows(grad)

    gain_sum, bias_sum = lax.fori_loop(0, blocks, norm_step, (wide_zero, wide_zero), unroll=2)
    total_out.go()
    rest_line = one_row(rest_up)
    up_columns_s[:LANES] = jnp.transpose(jnp.broadcast_to(one_row(main_up), (LANES, LANES)))
    up_columns_s[LANES:] = jnp.transpose(jnp.broadcast_to(rest_line + turn(rest_line), (LANES, LANES)))[:LOW]
    first_device = (place == 0).astype(F32)
    lines_s[...] = jnp.concatenate(
        [
            head_lines_ref[0:2],
            one_row(gain_sum),
            one_row(bias_sum),
            head_lines_ref[2:4],
            first_lines_ref[0:2] * first_device,
            jnp.zeros((8, D), F32),
        ],
        axis=0,
    )
    gate_at = KERNEL + 3
    lane = lax.broadcasted_iota(jnp.int32, (share, LANES), 1)
    for apart, pack_out in enumerate(packs):
        quarter = lax.bitwise_xor(stream, jnp.int32(apart))
        lanes = pl.ds(pl.multiple_of(quarter * LANES, LANES), LANES)
        pack_out[:LANES] = grad_up_s[LANES:, lanes].astype(BF16)
        pack_out[LANES:channels] = grad_up_s[LOW:LANES, lanes].astype(BF16)
        table = vectors_ref[pl.ds(pl.multiple_of(quarter * share, 8), share)]
        for other in range(2):
            at = pl.ds(pl.multiple_of((2 * lax.rem(quarter, 2) + other) * share, 8), share)
            column = jnp.where(
                quarter < quarters // 2, vectors_ref[at][:, gate_at : gate_at + 1], up_columns_s[at][:, 0:1]
            )
            table = jnp.where(lane == gate_at + other, column, table)
        pack_out[channels : channels + share] = table.astype(BF16)
        pack_out[channels + share :] = lines_s[:, lanes].astype(BF16)


def output_kernel(
    x_ref, mixed_ref, head_ref, down_ref, down_bias_ref, merge_ref, merge_bias_ref, out_ref, joined_out
):
    sources = mixed_ref.shape[0]
    rows = x_ref.shape[0]
    channels = HALF // sources
    share = channels // 4
    attn_parts = []
    branch_attn = jnp.zeros((rows, D), F32)
    branch_mlp = jnp.zeros((rows, D), F32)
    for source in range(sources):
        attn = turn(mixed_ref[source, :rows, LANES:].astype(F32))[:, :HEAD].astype(BF16)
        attn_parts.append(attn)
        branch_attn = branch_attn + dot_nn(attn, head_ref[source * HEAD : (source + 1) * HEAD])
        down = jnp.concatenate(
            [down_ref[(part * sources + source) * share : (part * sources + source + 1) * share] for part in range(4)],
            axis=0,
        )
        branch_mlp = branch_mlp + dot_nn(mixed_ref[source, :rows, :channels], down)
    joined = jnp.concatenate(
        [branch_attn.astype(BF16), (branch_mlp + line_of(down_bias_ref)).astype(BF16)], axis=1
    )
    result = x_ref[...].astype(F32) + dot_nn(joined, merge_ref[...]) + line_of(merge_bias_ref)
    out_ref[...] = result.astype(BF16)
    turned = jnp.transpose(joined.astype(F32))
    heads = jnp.transpose(jnp.concatenate(attn_parts, axis=1).astype(F32))
    merge_share = turned.shape[0] // (4 * sources)
    head_share = heads.shape[0] // (4 * sources)
    used = 4 * (merge_share + head_share)
    for target in range(sources):
        for part in range(4):
            at = (part * sources + target) * merge_share
            joined_out[target, part * merge_share : (part + 1) * merge_share] = turned[
                at : at + merge_share
            ].astype(BF16)
            at = (part * sources + target) * head_share
            to = 4 * merge_share + part * head_share
            joined_out[target, to : to + head_share] = heads[at : at + head_share].astype(BF16)
        joined_out[target, used:] = jnp.zeros((joined_out.shape[1] - used, rows), BF16)


def merge_kernel(joined_ref, branch_ref, cot_ref, up_0, up_1, up_2, up_3, pack_0, pack_1, pack_2, pack_3, merge_s, head_s):
    stream = lax.axis_index("stream")
    cot_ref = cot_ref()
    sources, _, rows = joined_ref.shape
    merge_rows = 2 * D // sources
    head_rows = D // sources
    grad_merge = jnp.zeros((merge_rows, D), F32)
    grad_head = jnp.zeros((head_rows, D), F32)
    for source in range(sources):
        at = slice(source * rows, (source + 1) * rows)
        joined = joined_ref[source]
        grad_merge = grad_merge + dot_nn(joined[:merge_rows], cot_ref[at])
        grad_head = grad_head + dot_nn(joined[merge_rows : merge_rows + head_rows], branch_ref[at])
    merge_s[...] = grad_merge
    head_s[...] = grad_head
    first = up_0.shape[0]
    ups = (up_0, up_1, up_2, up_3)
    for apart, pack_out in enumerate((pack_0, pack_1, pack_2, pack_3)):
        pack_out[:first] = ups[apart][...]
        quarter = lax.bitwise_xor(stream, jnp.int32(apart))
        for grad_s, base in ((merge_s, first), (head_s, first + merge_rows)):
            share = grad_s.shape[0] // 4
            at = pl.ds(pl.multiple_of(quarter * share, share), share)
            for tile in range(4):
                to = base + tile * share
                pack_out[to : to + share] = grad_s[at, tile * LANES : (tile + 1) * LANES].astype(BF16)


def frames_kernel(x_ref, cot_ref, total_ref, out_ref):
    for part in range(x_ref.shape[0] // 32):
        rows = slice(part * 32, part * 32 + 32)
        inputs = x_ref[rows].astype(F32)
        mean = jnp.mean(inputs, axis=-1, keepdims=True)
        centred = inputs - mean
        rate = lax.rsqrt(jnp.mean(centred * centred, axis=-1, keepdims=True) + EPS)
        hat = centred * rate
        grad = total_ref[0, rows].astype(F32)
        for source in range(1, total_ref.shape[0]):
            grad = grad + total_ref[source, rows].astype(F32)
        plain = jnp.mean(grad, axis=-1, keepdims=True)
        along = jnp.mean(grad * hat, axis=-1, keepdims=True)
        out_ref[rows] = cot_ref[rows].astype(F32) + rate * (grad - plain - hat * along)


def add_kernel(*refs):
    out_ref = refs[-1]
    first = 0
    for at in range(0, len(refs) - 1, 4):
        total = refs[at][...].astype(F32)
        for ref in refs[at + 1 : at + 4]:
            total = total + ref[...].astype(F32)
        out_ref[first : first + total.shape[0]] = total.astype(BF16)
        first += total.shape[0]


def gather_parts(part_refs, all_s):
    place = lax.axis_index("tm")
    for apart, part_ref in enumerate(part_refs):
        all_s[lax.bitwise_xor(jnp.int32(apart), place)] = part_ref[...]


def lines_from(all_s, base, size):
    return jnp.concatenate([all_s[source, base : base + size] for source in range(all_s.shape[0])], axis=0).astype(F32)


def early_kernel(*refs):
    qkv_out, pos_out, down_out, up_out, all_s = refs[HEADS:]
    gather_parts(refs[:HEADS], all_s)
    sources = all_s.shape[0]
    share = HALF // (4 * sources)
    for kind in range(4):
        lines = jnp.transpose(lines_from(all_s, kind * HEAD, HEAD))
        if kind < 3:
            qkv_out[:, kind * D : (kind + 1) * D] = lines
        else:
            pos_out[...] = lines
    base = 4 * HEAD
    for source in range(sources):
        for tile in range(4):
            down_out[source * share : (source + 1) * share, tile * LANES : (tile + 1) * LANES] = all_s[
                source, base + tile * share : base + (tile + 1) * share
            ].astype(F32)
    wide = sources * share
    for group in range(4):
        up_out.buffer[:, group * wide : (group + 1) * wide] = jnp.transpose(
            lines_from(all_s, base + 4 * share + group * share, share)
        )


def late_kernel(*refs):
    part_refs = refs[1 : HEADS + 1]
    (
        attn_gain_out,
        attn_bias_out,
        mlp_gain_out,
        mlp_bias_out,
        content_out,
        position_out,
        outw_out,
        up_out,
        up_bias_out,
        gain_out,
        bias_out,
        taps_out,
        conv_bias_out,
        down_bias_out,
        merge_out,
        merge_bias_out,
        all_s,
    ) = refs[HEADS + 1 :]
    gather_parts(part_refs, all_s)
    sources = all_s.shape[0]
    channels = HALF // sources
    share = channels // 4
    base = 0
    for group in range(4):
        at = group * sources * share
        up_out.buffer[:, at : at + sources * share] = jnp.transpose(lines_from(all_s, base + group * share, share))
    up_out.go()
    table = jnp.transpose(lines_from(all_s, base + channels, share))
    taps_out[...] = table[:KERNEL]
    conv_bias_out[...] = table[KERNEL]
    gain_out[...] = table[KERNEL + 1]
    bias_out[...] = table[KERNEL + 2]
    wide = sources * share
    up_bias_out[:wide] = table[KERNEL + 3]
    up_bias_out[wide:] = table[KERNEL + 4]
    base = base + channels + share
    lines = all_s[0, base : base + 16].astype(F32)
    for source in range(1, sources):
        lines = lines + all_s[source, base : base + 16].astype(F32)
    outs = (attn_gain_out, attn_bias_out, mlp_gain_out, mlp_bias_out, content_out, position_out, down_bias_out, merge_bias_out)
    for line, out in enumerate(outs):
        out[...] = lines[line]
    base = base + 16
    merge_share = 2 * D // (4 * sources)
    head_share = D // (4 * sources)
    for source in range(sources):
        for tile in range(4):
            lanes = slice(tile * LANES, (tile + 1) * LANES)
            at = base + tile * merge_share
            merge_out[source * merge_share : (source + 1) * merge_share, lanes] = all_s[
                source, at : at + merge_share
            ].astype(F32)
            at = base + 4 * merge_share + tile * head_share
            outw_out[source * head_share : (source + 1) * head_share, lanes] = all_s[
                source, at : at + head_share
            ].astype(F32)


def moved(block, axis, bits):
    count = lax.axis_size(axis)
    return lax.ppermute(block, axis, [(index, index ^ bits) for index in range(count)])


def over_streams(packs):
    return [packs[0]] + [moved(packs[bits], "stream", bits) for bits in range(1, lax.axis_size("stream"))]


def near_blocks(block):
    return [block] + [moved(block, "tm", bits) for bits in range(2, lax.axis_size("tm"), 2)]


def far_blocks(near):
    far = [moved(part, "tm", 1) for part in near]
    return [part for pair in zip(near, far) for part in pair]


def spread(block):
    return far_blocks(near_blocks(block))


def head_device(
    frames,
    lengths,
    cotangent,
    ln_attn_gain,
    ln_attn_bias,
    ln_mlp_gain,
    ln_mlp_bias,
    qkv_weight,
    content_bias,
    position_bias,
    pos_weight,
    out_weight,
    up_weight,
    up_bias,
    gate_norm_gain,
    gate_norm_bias,
    conv_kernel,
    conv_bias,
    down_weight,
    down_bias,
    merge_weight,
    merge_bias,
):
    count = lax.axis_size("tm")
    quarters = lax.axis_size("stream")
    own = frames.shape[1]
    total = own * count
    folded = total + total // 2
    padded = folded + 4 * MARGIN
    share = HALF // (quarters * count)
    channels = HALF // count
    quarter = D // quarters
    own_frames = frames[0]
    own_cotangent = cotangent[0]

    whole, late = Part(), Part(late=True)
    near = near_blocks(own_frames)
    cot_near = near_blocks(own_cotangent)
    up_own, table, qkv_own, pos_own, bias_own = kernel_call(
        select_kernel,
        [
            ((D, 3 * LANES), BF16),
            ((2, 8 + KERNEL + 1, LANES), F32),
            ((D, 3 * LANES), BF16),
            ((D, LANES), BF16),
            ((8, LANES), F32),
        ],
        10 * "v",
    )(
        up_weight,
        up_bias,
        gate_norm_gain,
        gate_norm_bias,
        conv_bias,
        conv_kernel,
        qkv_weight,
        pos_weight,
        content_bias,
        position_bias,
    )
    near, up_own = lax.optimization_barrier((near, up_own))
    blocks = far_blocks(near)
    frequency = jnp.exp(jnp.arange(D // 2, dtype=F32) * (-2.0 * math.log(10000.0) / D))
    coarse = jnp.arange(0, total, BLOCK, dtype=F32)[:, None] * frequency[None]
    fine = jnp.arange(BLOCK, dtype=F32)[:, None] * frequency[None]
    coarse_table = jnp.concatenate([jnp.sin(coarse), jnp.cos(coarse)], axis=1)
    fine_table = jnp.concatenate([jnp.sin(fine), jnp.cos(fine)], axis=1)

    n_attn, n_mlp, hat, q_position, query, key, value, prob, attn, row_share, stats = kernel_call(
        attend_kernel,
        [
            ((total, D), BF16, 1),
            ((total, D), BF16, 1),
            ((total, D), BF16, 1),
            ((total, LANES), BF16, 1),
            ((total, LANES + D), BF16, 1),
            ((total, LANES + D), BF16, 1),
            ((total, LANES), BF16, 1),
            ((total, total), BF16, 1),
            ((total, LANES), F32, 1),
            ((total, LANES), F32, 1),
            ((total, LANES), F32, 1),
        ],
        [
            "s",
            blocks_part(),
            *"vvvvvvvvv",
            Part((D, HALF), lambda refs, buffer: [(refs[0].at[:, pl.ds(HALF, HALF)], buffer)], late=True),
            "v",
        ],
        [((BLOCK, HALF), F32)],
        bounds=True,
    )(
        lengths,
        *blocks,
        ln_attn_gain,
        ln_attn_bias,
        ln_mlp_gain,
        ln_mlp_bias,
        qkv_own,
        pos_own,
        bias_own,
        coarse_table,
        fine_table,
        up_weight,
        up_bias,
    )

    n_mlp, cot_near = lax.optimization_barrier((n_mlp, cot_near))
    cot = far_blocks(cot_near)

    def own_down(refs, buffer):
        place = lax.axis_index("tm")
        stride = HALF // quarters
        return [
            (
                refs[0].at[pl.ds(pl.multiple_of(part * stride + share * place, 16), share)],
                buffer.at[pl.ds(part * share, share)],
            )
            for part in range(quarters)
        ]

    mixed, gate_pre, grad_y, slope, gate_hat, early_pack, vectors, first_lines = kernel_call(
        mlp_first_kernel,
        [
            ((count, own + 16, 2 * LANES), BF16, 1),
            ((folded, LANES), BF16, 1),
            ((folded, LANES), BF16, 1),
            ((folded, LANES), BF16, 1),
            ((folded, LANES), BF16, 1),
            ((quarters, 8 * share, LANES), BF16, 1),
            ((channels, LANES), F32),
            ((8, D), F32),
        ],
        [
            "s",
            whole,
            "v",
            "v",
            whole,
            blocks_part(late=True),
            rows_part(D, D, late=True),
            Part((2 * LANES, D), own_down, late=True),
            Part(late=True),
        ],
        [
            ((folded, LANES), F32),
            ((folded, LANES), F32),
            ((total, 2 * LANES), BF16),
            ((folded, LANES), F32),
            ((folded, LANES), F32),
            ((padded, LANES), F32),
            ((padded, LANES), F32),
            ((folded, LANES), F32),
            ((folded, LANES), F32),
            ((total, D), BF16),
            ((total, 2 * LANES), BF16),
            ((2, 32, 8, LANES), F32),
            ((2, 32, 8, LANES), F32),
            ((2, 32, 8, LANES), F32),
            ((total, LANES), F32),
            ((3, WINDOW + 2 * MARGIN, LANES), F32),
            ((3, WINDOW + 2 * MARGIN, LANES), F32),
        ],
        bounds=True,
    )(lengths, n_mlp, up_own, table, stats, *cot, merge_weight, down_weight, attn)
    mixed_own = lax.all_to_all(mixed, "tm", 0, 0, tiled=True)

    def own_head(refs, buffer):
        at = pl.ds(pl.multiple_of(lax.axis_index("tm") * HEAD, HEAD), HEAD)
        return [(refs[0].at[at], buffer.at[pl.ds(0, HEAD)])]

    branch, from_attn, *head_packs, head_lines = kernel_call(
        attend_back_kernel,
        [
            ((total, D), BF16, 1),
            ((total, D), BF16, 1),
            *([((4 * HEAD + 8 * share, LANES), BF16, 1)] * quarters),
            ((8, D), F32),
        ],
        [
            blocks_part(),
            rows_part(0, D),
            Part((LANES, D), own_head),
            whole,
            late,
            late,
            late,
            late,
            "v",
            "v",
            late,
            Part((total, LANES), lambda refs, buffer: [(refs[0].at[:, pl.ds(0, LANES)], buffer)], late=True),
            late,
            late,
            late,
            late,
            "v",
            late,
        ],
        [
            ((total, LANES), BF16),
            ((total, total), BF16),
            ((total, D), BF16),
            ((total, 3 * LANES), BF16),
            ((4 * HEAD, D), F32),
        ],
    )(
        *cot,
        merge_weight,
        out_weight,
        row_share,
        value,
        attn,
        prob,
        key,
        coarse_table,
        fine_table,
        pos_own,
        query,
        n_attn,
        q_position,
        qkv_own,
        hat,
        ln_attn_gain,
        early_pack,
    )
    head_parts = over_streams(head_packs)
    mixed_own, _ = lax.optimization_barrier((mixed_own, head_lines))
    out_rows, joined = kernel_call(
        output_kernel,
        [((own, D), BF16), ((count, 256, own), BF16)],
        "vvvvvvv",
        megas=24,
    )(own_frames, mixed_own, out_weight, down_weight, down_bias, merge_weight, merge_bias)
    joined_all = lax.all_to_all(joined, "tm", 0, 0, tiled=True)
    gate_pre, _ = lax.optimization_barrier((gate_pre, joined))
    up_rows = 5 * share + 16
    from_both, *up_packs = kernel_call(
        mlp_second_kernel,
        [((count, own, D), BF16, 1)] + [((up_rows, LANES), BF16)] * quarters,
        [
            Part(
                (count, 2 * total // BLOCK, 2 * LANES),
                lambda refs, buffer: [(refs[0].at[:, pl.ds(own, 2 * total // BLOCK)], buffer)],
            ),
            *([whole] * 4),
            late,
            late,
            "v",
            late,
            late,
            *"vvv",
        ],
        [
            ((total, 3 * LANES), BF16),
            ((total, LANES), F32),
            ((2 * LANES, D), F32),
            ((16, D), F32),
            ((channels, LANES), F32),
        ],
    )(
        mixed_own,
        gate_pre,
        grad_y,
        slope,
        gate_hat,
        up_own,
        hat,
        ln_mlp_gain,
        from_attn,
        n_mlp,
        vectors,
        first_lines,
        head_lines,
    )
    joined_all, head_parts, up_packs = lax.optimization_barrier((joined_all, head_parts, up_packs))
    late_rows = up_rows + 3 * D // count
    late_packs = kernel_call(
        merge_kernel,
        [((late_rows, LANES), BF16)] * quarters,
        ["v", "v", blocks_part(), *"vvvv"],
        [((2 * D // count, D), F32), ((D // count, D), F32)],
        megas=24,
    )(joined_all, branch, *cot, *up_packs)
    late_moved = over_streams(late_packs)
    from_both, head_parts, _ = lax.optimization_barrier((from_both, head_parts, late_packs[0]))
    from_all = lax.all_to_all(from_both, "tm", 0, 0, tiled=True)
    (early_part,) = kernel_call(add_kernel, [((4 * HEAD + 8 * share, LANES), BF16)], quarters * "v", megas=24)(
        *head_parts
    )
    early_near = near_blocks(early_part)
    late_moved, early_part = lax.optimization_barrier((late_moved, early_part))
    (late_part,) = kernel_call(add_kernel, [((late_rows, LANES), BF16)], quarters * "v", megas=24)(*late_moved)
    late_near = near_blocks(late_part)
    early_all = far_blocks(early_near)
    late_parts = far_blocks(late_near)
    (grad_frames,) = kernel_call(frames_kernel, [((own, D), F32)], "vvv", megas=24)(
        own_frames, own_cotangent, from_all
    )
    grad_qkv, grad_pos, grad_down, half_up = kernel_call(
        early_kernel,
        [
            ((quarter, 3 * D), F32),
            ((quarter, D), F32),
            ((HALF // quarters, D), F32),
            ((quarter, 2 * HALF), F32, 1, (quarter, HALF), lambda ref: ref.at[:, pl.ds(0, HALF)]),
        ],
        count * "v",
        [((count, 4 * HEAD + 8 * share, LANES), BF16)],
        megas=24,
    )(*early_all)
    late_parts, grad_frames = lax.optimization_barrier((late_parts, grad_frames))
    late = kernel_call(
        late_kernel,
        [((quarter,), F32)] * 6
        + [
            ((quarter, D), F32),
            ((quarter, 2 * HALF), F32, 1, (quarter, HALF), lambda ref: ref.at[:, pl.ds(HALF, HALF)]),
            ((2 * HALF // quarters,), F32),
            ((HALF // quarters,), F32),
            ((HALF // quarters,), F32),
            ((KERNEL, HALF // quarters), F32),
            ((HALF // quarters,), F32),
            ((quarter,), F32),
            ((2 * D // quarters, D), F32),
            ((quarter,), F32),
        ],
        "k" + count * "v",
        [((count,) + late_part.shape, BF16)],
        megas=24,
        aliases={0: 7},
    )(half_up, *late_parts)
    return (
        out_rows[None],
        grad_frames[None],
        *late[:4],
        grad_qkv,
        *late[4:6],
        grad_pos,
        *late[6:13],
        grad_down,
        *late[13:],
    )


def per_device(*operands):
    fits = (
        lax.axis_size("tm") == HEADS
        and lax.axis_size("stream") * LANES == D
        and operands[0].shape[1] == BLOCK
    )
    return head_device(*operands) if fits else frame_device(*operands)


def solution(mesh):
    return jax.shard_map(
        per_device,
        mesh=mesh,
        in_specs=(
            P("stream", "tm", None),
            P("stream", None),
            P("stream", "tm", None),
            P(),
            P(),
            P(),
            P(),
            P(),
            P(),
            P(),
            P(),
            P(),
            P(),
            P(),
            P(),
            P(),
            P(),
            P(),
            P(),
            P(),
            P(),
            P(),
        ),
        out_specs=(
            P("stream", "tm", None),
            P("stream", "tm", None),
            P("stream"),
            P("stream"),
            P("stream"),
            P("stream"),
            P("stream", None),
            P("stream"),
            P("stream"),
            P("stream", None),
            P("stream", None),
            P("stream", None),
            P("stream"),
            P("stream"),
            P("stream"),
            P(None, "stream"),
            P("stream"),
            P("stream", None),
            P("stream"),
            P("stream", None),
            P("stream"),
        ),
        check_vma=False,
    )
```

```python
import math

import jax
import jax.numpy as jnp
from jax import lax
from jax.experimental import pallas as pl
from jax.experimental.pallas import tpu as pltpu
from jax.sharding import PartitionSpec as P

D = 512
HEADS = 8
HEAD = 64
KERNEL = 31
ITEMS = 5
HALF = 1536


EPS = 1e-05
MASKED = -1e30


def extended(block, sides, width):
    for axis, dim in sides:
        count = lax.axis_size(axis)
        forward = [(i, i + 1) for i in range(count - 1)]
        backward = [(target, source) for source, target in forward]
        low = lax.ppermute(
            lax.slice_in_dim(block, block.shape[dim] - width, None, axis=dim), axis, forward
        )
        high = lax.ppermute(lax.slice_in_dim(block, 0, width, axis=dim), axis, backward)
        block = jnp.concatenate([low, block, high], axis=dim)
    return block


def norm_rows(inputs, scale_row, shift_row):
    row_mean = jnp.mean(inputs, axis=-1, keepdims=True)
    centred = inputs - row_mean
    spread = jnp.mean(centred * centred, axis=-1, keepdims=True)
    return centred * lax.rsqrt(spread + EPS) * scale_row + shift_row


def gelu_exact(inputs):
    return jax.nn.gelu(inputs, approximate=False)


def frame_info(lengths, offset, extent):
    item_ends = jnp.cumsum(lengths)
    first_table = jnp.concatenate([item_ends - lengths, item_ends[-1:]])
    frame_index = offset + jnp.arange(extent, dtype=jnp.int32)
    item_of = jnp.sum((frame_index[:, None] >= item_ends[None, :]).astype(jnp.int32), axis=1)
    labels = jnp.arange(ITEMS + 1, dtype=jnp.int32)
    first_frame = jnp.sum(
        jnp.where(item_of[:, None] == labels[None, :], first_table[None, :], 0), axis=1
    )
    return (frame_index, item_of, frame_index - first_frame)


def angles(place_in):
    frequency = jnp.exp(jnp.arange(D // 2, dtype=jnp.float32) * (-2.0 * math.log(10000.0) / D))
    phase_angle = place_in.astype(jnp.float32)[:, None] * frequency[None, :]
    return (jnp.sin(phase_angle), jnp.cos(phase_angle))


def rel_query(projected, sine_rows, cosine_rows):
    half_size = projected.shape[-1] // 2
    first_half = projected[..., :half_size]
    second_half = projected[..., half_size:]
    sine_wide = sine_rows[:, None, :]
    cosine_wide = cosine_rows[:, None, :]
    return jnp.concatenate(
        [
            first_half * sine_wide + second_half * cosine_wide,
            second_half * sine_wide - first_half * cosine_wide,
        ],
        axis=-1,
    )


def step_size(extent):
    return math.gcd(extent, 512)


def score_block(q_content, q_rel, query_item, query_frame, key_block, key_start, lengths):
    extent = key_block.shape[0]
    key_frame, key_item, key_place = frame_info(lengths, key_start, extent)
    sine_rows, cosine_rows = angles(key_place)
    k_rel = jnp.concatenate([cosine_rows, sine_rows], axis=1).astype(jnp.bfloat16)
    raw_scores = jnp.einsum(
        "qhe,khe->hqk",
        q_content,
        key_block.reshape(extent, HEADS, HEAD),
        preferred_element_type=jnp.float32,
    )
    raw_scores = raw_scores + jnp.einsum(
        "qhc,kc->hqk", q_rel, k_rel, preferred_element_type=jnp.float32
    )
    allowed = (query_item[:, None] == key_item[None, :]) & (
        (query_item[:, None] < ITEMS) | (query_frame[:, None] == key_frame[None, :])
    )
    return (raw_scores, allowed, k_rel)


def block_grads(
    q_content,
    q_rel,
    query_item,
    query_frame,
    grad_out,
    log_total,
    delta_rows,
    key_block,
    value_block,
    key_start,
    lengths,
):
    extent = key_block.shape[0]
    raw_scores, allowed, k_rel = score_block(
        q_content, q_rel, query_item, query_frame, key_block, key_start, lengths
    )
    prob_rows = jnp.where(allowed[None], jnp.exp(raw_scores * 0.125 - log_total[:, :, None]), 0.0)
    grad_prob = jnp.einsum(
        "qhe,khe->hqk",
        grad_out,
        value_block.reshape(extent, HEADS, HEAD),
        preferred_element_type=jnp.float32,
    )
    grad_raw = (prob_rows * (grad_prob - delta_rows[:, :, None]) * 0.125).astype(jnp.bfloat16)
    return (prob_rows.astype(jnp.bfloat16), grad_raw, k_rel)


def frame_device(
    frames,
    lengths,
    cotangent,
    ln_attn_gain,
    ln_attn_bias,
    ln_mlp_gain,
    ln_mlp_bias,
    qkv_weight,
    content_bias,
    position_bias,
    pos_weight,
    out_weight,
    up_weight,
    up_bias,
    gate_norm_gain,
    gate_norm_bias,
    conv_kernel,
    conv_bias,
    down_weight,
    down_bias,
    merge_weight,
    merge_bias,
):
    row_count = frames.shape[1]
    cycle_size = lax.axis_size("tm")
    offset = lax.axis_index("tm") * row_count
    stream_lengths = lengths[0]
    inputs = frames[0].astype(jnp.float32)
    frame_index, item_of, place_in = frame_info(stream_lengths, offset, row_count)
    sine_rows, cosine_rows = angles(place_in)
    attn_norm, attn_pull = jax.vjp(
        norm_rows, inputs, ln_attn_gain.astype(jnp.float32), ln_attn_bias.astype(jnp.float32)
    )
    mlp_norm, mlp_pull = jax.vjp(
        norm_rows, inputs, ln_mlp_gain.astype(jnp.float32), ln_mlp_bias.astype(jnp.float32)
    )
    attn_norm_low = attn_norm.astype(jnp.bfloat16)
    mlp_norm_low = mlp_norm.astype(jnp.bfloat16)
    qkv_rows = jnp.dot(attn_norm_low, qkv_weight, preferred_element_type=jnp.float32)
    query_rows = qkv_rows[:, :D]
    key_rows = qkv_rows[:, D : 2 * D].astype(jnp.bfloat16)
    value_rows = qkv_rows[:, 2 * D :].astype(jnp.bfloat16)
    q_content = (query_rows + content_bias.astype(jnp.float32)).astype(jnp.bfloat16)
    q_position = (query_rows + position_bias.astype(jnp.float32)).astype(jnp.bfloat16)
    content_heads = q_content.reshape(row_count, HEADS, HEAD)
    position_heads = q_position.reshape(row_count, HEADS, HEAD)
    pos_heads = pos_weight.reshape(D, HEADS, HEAD)
    projected = jnp.einsum(
        "the,che->thc", position_heads, pos_heads, preferred_element_type=jnp.float32
    )
    q_rel = rel_query(projected, sine_rows, cosine_rows).astype(jnp.bfloat16)
    start_state = (
        jnp.full((HEADS, row_count), MASKED, jnp.float32),
        jnp.zeros((HEADS, row_count), jnp.float32),
        jnp.zeros((HEADS, row_count, HEAD), jnp.float32),
    )
    fold_state = start_state
    key_piece = lax.all_gather(key_rows, "tm", axis=0, tiled=True)
    value_piece = lax.all_gather(value_rows, "tm", axis=0, tiled=True)
    extent = key_piece.shape[0]
    step_rows = step_size(extent)

    def forward_one_step(inner_state, step_index):
        row_top, row_total, row_acc = inner_state
        key_block = lax.dynamic_slice_in_dim(key_piece, step_index * step_rows, step_rows, 0)
        value_block = lax.dynamic_slice_in_dim(value_piece, step_index * step_rows, step_rows, 0)
        raw_scores, allowed, k_rel = score_block(
            content_heads,
            q_rel,
            item_of,
            frame_index,
            key_block,
            step_index * step_rows,
            stream_lengths,
        )
        scaled = jnp.where(allowed[None], raw_scores * 0.125, MASKED)
        new_top = jnp.maximum(row_top, jnp.max(scaled, axis=2))
        weight = jnp.where(allowed[None], jnp.exp(scaled - new_top[:, :, None]), 0.0)
        factor = jnp.exp(row_top - new_top)
        row_total = row_total * factor + jnp.sum(weight, axis=2)
        row_acc = row_acc * factor[:, :, None] + jnp.einsum(
            "hqk,khe->hqe",
            weight.astype(jnp.bfloat16),
            value_block.reshape(step_rows, HEADS, HEAD),
            preferred_element_type=jnp.float32,
        )
        return ((new_top, row_total, row_acc), None)

    fold_state, unused = lax.scan(
        forward_one_step, fold_state, jnp.arange(extent // step_rows, dtype=jnp.int32)
    )
    row_top, row_total, row_acc = fold_state
    attn_heads = row_acc / row_total[:, :, None]
    log_total = row_top + jnp.log(row_total)
    attn_low = jnp.transpose(attn_heads, (1, 0, 2)).reshape(row_count, D).astype(jnp.bfloat16)
    branch_attn = jnp.dot(attn_low, out_weight, preferred_element_type=jnp.float32).astype(
        jnp.bfloat16
    )
    hidden_pre = jnp.dot(
        mlp_norm_low, up_weight, preferred_element_type=jnp.float32
    ) + up_bias.astype(jnp.float32)
    hidden, gelu_pull = jax.vjp(gelu_exact, hidden_pre)
    gate_half = hidden[:, :HALF]
    conv_norm, conv_pull = jax.vjp(
        norm_rows,
        hidden[:, HALF:],
        gate_norm_gain.astype(jnp.float32),
        gate_norm_bias.astype(jnp.float32),
    )
    conv_in = conv_norm.astype(jnp.bfloat16)
    half_width = KERNEL // 2
    conv_wide = extended(conv_in, (("tm", 0),), half_width)
    wide_frame, wide_item, wide_place = frame_info(
        stream_lengths, offset - half_width, row_count + 2 * half_width
    )
    kernel_rows = conv_kernel.astype(jnp.float32)
    conv_out = conv_bias.astype(jnp.float32) + jnp.zeros_like(gate_half)
    for tap_index in range(KERNEL):
        same_item = (wide_item[tap_index : tap_index + row_count] == item_of)[:, None]
        conv_out = (
            conv_out
            + jnp.where(
                same_item, conv_wide[tap_index : tap_index + row_count].astype(jnp.float32), 0.0
            )
            * kernel_rows[tap_index]
        )
    gated_low = (gate_half * conv_out).astype(jnp.bfloat16)
    branch_mlp = (
        jnp.dot(gated_low, down_weight, preferred_element_type=jnp.float32)
        + down_bias.astype(jnp.float32)
    ).astype(jnp.bfloat16)
    joined = jnp.concatenate([branch_attn, branch_mlp], axis=1)
    result = (
        inputs
        + jnp.dot(joined, merge_weight, preferred_element_type=jnp.float32)
        + merge_bias.astype(jnp.float32)
    )
    out_rows = result.astype(jnp.bfloat16)[None]
    grad_low = cotangent[0]
    grad_rows = grad_low.astype(jnp.float32)
    grad_merge_bias = jnp.sum(grad_rows, axis=0)
    grad_merge_weight = jnp.einsum(
        "tc,td->cd", joined, grad_low, preferred_element_type=jnp.float32
    )
    grad_joined = jnp.einsum(
        "td,cd->tc", grad_low, merge_weight, preferred_element_type=jnp.float32
    )
    grad_attn_branch = grad_joined[:, :D].astype(jnp.bfloat16)
    grad_mlp_branch = grad_joined[:, D:].astype(jnp.bfloat16)
    grad_down_weight = jnp.einsum(
        "tc,td->cd", gated_low, grad_mlp_branch, preferred_element_type=jnp.float32
    )
    grad_down_bias = jnp.sum(grad_mlp_branch.astype(jnp.float32), axis=0)
    grad_gated = jnp.einsum(
        "td,cd->tc", grad_mlp_branch, down_weight, preferred_element_type=jnp.float32
    )
    grad_gate_half = grad_gated * conv_out
    grad_conv_out = (grad_gated * gate_half).astype(jnp.bfloat16)
    grad_conv_rows = grad_conv_out.astype(jnp.float32)
    grad_conv_bias = jnp.sum(grad_conv_rows, axis=0)
    grad_wide = extended(grad_conv_out, (("tm", 0),), half_width)
    kernel_list = []
    grad_conv_in = jnp.zeros_like(grad_conv_rows)
    for tap_index in range(KERNEL):
        same_item = (wide_item[tap_index : tap_index + row_count] == item_of)[:, None]
        kernel_list.append(
            jnp.sum(
                jnp.where(
                    same_item, conv_wide[tap_index : tap_index + row_count].astype(jnp.float32), 0.0
                )
                * grad_conv_rows,
                axis=0,
            )
        )
        back_start = 2 * half_width - tap_index
        back_item = (wide_item[back_start : back_start + row_count] == item_of)[:, None]
        grad_conv_in = (
            grad_conv_in
            + jnp.where(
                back_item, grad_wide[back_start : back_start + row_count].astype(jnp.float32), 0.0
            )
            * kernel_rows[tap_index]
        )
    grad_conv_kernel = jnp.stack(kernel_list)
    grad_second, grad_gate_norm_gain, grad_gate_norm_bias = conv_pull(grad_conv_in)
    (grad_pre_rows,) = gelu_pull(jnp.concatenate([grad_gate_half, grad_second], axis=1))
    grad_pre = grad_pre_rows.astype(jnp.bfloat16)
    grad_up_bias = jnp.sum(grad_pre.astype(jnp.float32), axis=0)
    grad_up_weight = jnp.einsum(
        "tc,tf->cf", mlp_norm_low, grad_pre, preferred_element_type=jnp.float32
    )
    grad_mlp_norm = jnp.einsum("tf,cf->tc", grad_pre, up_weight, preferred_element_type=jnp.float32)
    grad_out_weight = jnp.einsum(
        "tc,td->cd", attn_low, grad_attn_branch, preferred_element_type=jnp.float32
    )
    grad_attn_low = jnp.einsum(
        "td,cd->tc", grad_attn_branch, out_weight, preferred_element_type=jnp.float32
    ).astype(jnp.bfloat16)
    grad_out_heads = grad_attn_low.reshape(row_count, HEADS, HEAD)
    delta_rows = jnp.sum(
        jnp.transpose(grad_out_heads.astype(jnp.float32), (1, 0, 2)) * attn_heads, axis=2
    )
    total_frames = row_count * cycle_size
    back_start_state = (
        jnp.zeros((row_count, HEADS, HEAD), jnp.float32),
        jnp.zeros((row_count, HEADS, D), jnp.float32),
        jnp.zeros((total_frames, D), jnp.float32),
        jnp.zeros((total_frames, D), jnp.float32),
    )
    back_key_piece = lax.all_gather(key_rows, "tm", axis=0, tiled=True)
    back_value_piece = lax.all_gather(value_rows, "tm", axis=0, tiled=True)
    extent = back_key_piece.shape[0]
    back_step_rows = step_size(extent)

    def back_one_step(inner_state, step_index):
        grad_content, grad_rel = inner_state
        key_block = lax.dynamic_slice_in_dim(
            back_key_piece, step_index * back_step_rows, back_step_rows, 0
        )
        value_block = lax.dynamic_slice_in_dim(
            back_value_piece, step_index * back_step_rows, back_step_rows, 0
        )
        prob_low, grad_raw, k_rel = block_grads(
            content_heads,
            q_rel,
            item_of,
            frame_index,
            grad_out_heads,
            log_total,
            delta_rows,
            key_block,
            value_block,
            step_index * back_step_rows,
            stream_lengths,
        )
        grad_content = grad_content + jnp.einsum(
            "hqk,khe->qhe",
            grad_raw,
            key_block.reshape(back_step_rows, HEADS, HEAD),
            preferred_element_type=jnp.float32,
        )
        grad_rel = grad_rel + jnp.einsum(
            "hqk,kc->qhc", grad_raw, k_rel, preferred_element_type=jnp.float32
        )
        key_part = jnp.einsum(
            "hqk,qhe->khe", grad_raw, content_heads, preferred_element_type=jnp.float32
        ).reshape(back_step_rows, D)
        value_part = jnp.einsum(
            "hqk,qhe->khe", prob_low, grad_out_heads, preferred_element_type=jnp.float32
        ).reshape(back_step_rows, D)
        return ((grad_content, grad_rel), (key_part, value_part))

    inner_state, block_parts = lax.scan(
        back_one_step,
        (back_start_state[0], back_start_state[1]),
        jnp.arange(extent // back_step_rows, dtype=jnp.int32),
    )
    key_all = block_parts[0].reshape(extent, D)
    value_all = block_parts[1].reshape(extent, D)
    grad_content, grad_rel, key_all, value_all = (
        inner_state[0],
        inner_state[1],
        key_all,
        value_all,
    )
    grad_keys, grad_values = (
        lax.psum_scatter(key_all, "tm", scatter_dimension=0, tiled=True),
        lax.psum_scatter(value_all, "tm", scatter_dimension=0, tiled=True),
    )
    half_size = D // 2
    rel_first = grad_rel[..., :half_size]
    rel_second = grad_rel[..., half_size:]
    sine_wide = sine_rows[:, None, :]
    cosine_wide = cosine_rows[:, None, :]
    grad_projected = jnp.concatenate(
        [
            rel_first * sine_wide - rel_second * cosine_wide,
            rel_first * cosine_wide + rel_second * sine_wide,
        ],
        axis=-1,
    ).astype(jnp.bfloat16)
    grad_pos_weight = jnp.einsum(
        "thc,the->che", grad_projected, position_heads, preferred_element_type=jnp.float32
    ).reshape(D, D)
    grad_q_position = jnp.einsum(
        "thc,che->the", grad_projected, pos_heads, preferred_element_type=jnp.float32
    )
    grad_content_bias = jnp.sum(grad_content, axis=0).reshape(D)
    grad_position_bias = jnp.sum(grad_q_position, axis=0).reshape(D)
    grad_query = (grad_content + grad_q_position).reshape(row_count, D).astype(jnp.bfloat16)
    grad_qkv = jnp.concatenate(
        [grad_query, grad_keys.astype(jnp.bfloat16), grad_values.astype(jnp.bfloat16)], axis=1
    )
    grad_qkv_weight = jnp.einsum(
        "tc,tf->cf", attn_norm_low, grad_qkv, preferred_element_type=jnp.float32
    )
    grad_attn_norm = jnp.einsum(
        "tf,cf->tc", grad_qkv, qkv_weight, preferred_element_type=jnp.float32
    )
    grad_from_attn, grad_ln_attn_gain, grad_ln_attn_bias = attn_pull(grad_attn_norm)
    grad_from_mlp, grad_ln_mlp_gain, grad_ln_mlp_bias = mlp_pull(grad_mlp_norm)
    grad_inputs = grad_rows + grad_from_attn + grad_from_mlp
    weight_grads = (
        grad_ln_attn_gain,
        grad_ln_attn_bias,
        grad_ln_mlp_gain,
        grad_ln_mlp_bias,
        grad_qkv_weight,
        grad_content_bias,
        grad_position_bias,
        grad_pos_weight,
        grad_out_weight,
        grad_up_weight,
        grad_up_bias,
        grad_gate_norm_gain,
        grad_gate_norm_bias,
        grad_conv_kernel,
        grad_conv_bias,
        grad_down_weight,
        grad_down_bias,
        grad_merge_weight,
        grad_merge_bias,
    )
    summed = lax.psum(
        (
            weight_grads[0],
            weight_grads[1],
            weight_grads[2],
            weight_grads[3],
            weight_grads[4],
            weight_grads[5],
            weight_grads[6],
            weight_grads[7],
            weight_grads[8],
            weight_grads[9],
            weight_grads[10],
            weight_grads[11],
            weight_grads[12],
            weight_grads[13],
            weight_grads[14],
            weight_grads[15],
            weight_grads[16],
            weight_grads[17],
            weight_grads[18],
        ),
        "tm",
    )
    shares = (
        lax.psum_scatter(
            summed[0].astype(jnp.bfloat16), "stream", scatter_dimension=0, tiled=True
        ).astype(jnp.float32),
        lax.psum_scatter(
            summed[1].astype(jnp.bfloat16), "stream", scatter_dimension=0, tiled=True
        ).astype(jnp.float32),
        lax.psum_scatter(
            summed[2].astype(jnp.bfloat16), "stream", scatter_dimension=0, tiled=True
        ).astype(jnp.float32),
        lax.psum_scatter(
            summed[3].astype(jnp.bfloat16), "stream", scatter_dimension=0, tiled=True
        ).astype(jnp.float32),
        lax.psum_scatter(
            summed[4].astype(jnp.bfloat16), "stream", scatter_dimension=0, tiled=True
        ).astype(jnp.float32),
        lax.psum_scatter(
            summed[5].astype(jnp.bfloat16), "stream", scatter_dimension=0, tiled=True
        ).astype(jnp.float32),
        lax.psum_scatter(
            summed[6].astype(jnp.bfloat16), "stream", scatter_dimension=0, tiled=True
        ).astype(jnp.float32),
        lax.psum_scatter(
            summed[7].astype(jnp.bfloat16), "stream", scatter_dimension=0, tiled=True
        ).astype(jnp.float32),
        lax.psum_scatter(
            summed[8].astype(jnp.bfloat16), "stream", scatter_dimension=0, tiled=True
        ).astype(jnp.float32),
        lax.psum_scatter(
            summed[9].astype(jnp.bfloat16), "stream", scatter_dimension=0, tiled=True
        ).astype(jnp.float32),
        lax.psum_scatter(
            summed[10].astype(jnp.bfloat16), "stream", scatter_dimension=0, tiled=True
        ).astype(jnp.float32),
        lax.psum_scatter(
            summed[11].astype(jnp.bfloat16), "stream", scatter_dimension=0, tiled=True
        ).astype(jnp.float32),
        lax.psum_scatter(
            summed[12].astype(jnp.bfloat16), "stream", scatter_dimension=0, tiled=True
        ).astype(jnp.float32),
        lax.psum_scatter(
            summed[13].astype(jnp.bfloat16), "stream", scatter_dimension=1, tiled=True
        ).astype(jnp.float32),
        lax.psum_scatter(
            summed[14].astype(jnp.bfloat16), "stream", scatter_dimension=0, tiled=True
        ).astype(jnp.float32),
        lax.psum_scatter(
            summed[15].astype(jnp.bfloat16), "stream", scatter_dimension=0, tiled=True
        ).astype(jnp.float32),
        lax.psum_scatter(
            summed[16].astype(jnp.bfloat16), "stream", scatter_dimension=0, tiled=True
        ).astype(jnp.float32),
        lax.psum_scatter(
            summed[17].astype(jnp.bfloat16), "stream", scatter_dimension=0, tiled=True
        ).astype(jnp.float32),
        lax.psum_scatter(
            summed[18].astype(jnp.bfloat16), "stream", scatter_dimension=0, tiled=True
        ).astype(jnp.float32),
    )
    return (out_rows, grad_inputs[None]) + tuple(shares)


LANES = 128
LOW = LANES // 2
BLOCK = 128
TALL = 256
WINDOW = 64
MARGIN = 16
BOUNDS = 16
MEGA = 1024 * 1024
F32 = jnp.float32
BF16 = jnp.bfloat16


def dot_nn(left, right):
    return jnp.dot(left, right, preferred_element_type=F32)


def dot_nt(left, right):
    return lax.dot_general(left, right, (((1,), (1,)), ((), ())), preferred_element_type=F32)


def dot_tn(left, right):
    return lax.dot_general(left, right, (((0,), (0,)), ((), ())), preferred_element_type=F32)


def rows_of(index, size, base=0):
    return pl.ds(pl.multiple_of(index * size, size) + base, size)


def line_of(ref):
    return ref[...].astype(F32).reshape(1, ref.shape[0])


def fold_rows(values):
    return jnp.sum(values.reshape(values.shape[0] // 8, 8, values.shape[1]), axis=0)


def one_row(values):
    return jnp.sum(values, axis=0, keepdims=True)


def turn(values):
    return pltpu.roll(values, LOW, 1)


def low_lanes(rows):
    return lax.broadcasted_iota(jnp.int32, (rows, LANES), 1) < LOW


def centre_rows(inputs):
    mean = jnp.mean(inputs, axis=-1, keepdims=True)
    centred = inputs - mean
    spread = jnp.mean(centred * centred, axis=-1, keepdims=True)
    return centred * lax.rsqrt(spread + EPS)


def gelu_parts(values):
    phi = 0.5 + 0.5 * lax.erf(values * math.sqrt(0.5))
    bell = jnp.exp(values * values * -0.5)
    return values * phi, phi + values * bell * (1.0 / math.sqrt(2.0 * math.pi))


class Part:
    def __init__(self, shape=None, pairs=None, refs=1, late=False):
        self.shape, self.pairs, self.refs, self.late = shape, pairs, refs, late

    def buffer(self, operand):
        return self.shape or operand.shape

    def copies(self, refs, buffer):
        return self.pairs(refs, buffer) if self.pairs else [(refs[0], buffer)]


def blocks_part(late=False):
    def pairs(refs, buffer):
        place = lax.axis_index("tm")
        return [
            (ref, buffer.at[rows_of(lax.bitwise_xor(jnp.int32(apart), place), BLOCK)])
            for apart, ref in enumerate(refs)
        ]

    return Part((HEADS * BLOCK, D), pairs, HEADS, late)


def rows_part(first, size, late=False):
    return Part((size, D), lambda refs, buffer: [(refs[0].at[pl.ds(first, size)], buffer)], late=late)


class Fetch:
    def __init__(self, pairs, buffer, sems, first):
        self.buffer, self.begun = buffer, False
        self.pending = [
            pltpu.make_async_copy(source, target, sems.at[first + index])
            for index, (source, target) in enumerate(pairs)
        ]

    def begin(self):
        if not self.begun:
            for copy in self.pending:
                copy.start()
        self.begun = True

    def __call__(self):
        self.begin()
        for copy in self.pending:
            copy.wait()
        self.pending = []
        return self.buffer


def begin(*fetches):
    for fetch in fetches:
        fetch.begin()


class Send:
    def __init__(self, buffer, target, sems):
        self.buffer, self.target, self.sems, self.copies = buffer, target, sems, []

    def go(self, *index):
        source, target = (self.buffer.at[index], self.target.at[index]) if index else (self.buffer, self.target)
        copy = pltpu.make_async_copy(source, target, self.sems[len(self.copies)])
        copy.start()
        self.copies.append(copy)

    def finish(self):
        if not self.copies:
            self.go()


SPACES = {"v": pltpu.VMEM, "s": pltpu.SMEM, "k": pl.ANY}


def kernel_call(body, out_shapes, plan, scratch=(), megas=58, bounds=False, aliases=None):
    def call(*operands):
        in_specs, buffers, at = [], [], 0
        for item in plan:
            if item == "f":
                in_specs.append(pl.BlockSpec(memory_space=pl.ANY))
                buffers.append(pltpu.VMEM(operands[at].shape, operands[at].dtype))
                at += 1
            elif isinstance(item, Part):
                in_specs += [pl.BlockSpec(memory_space=pl.ANY)] * item.refs
                buffers.append(pltpu.VMEM(item.buffer(operands[at]), operands[at].dtype))
                at += item.refs
            else:
                in_specs.append(pl.BlockSpec(memory_space=SPACES[item]))
                at += 1
        sent = [out for out in out_shapes if len(out) > 2]
        buffers += [pltpu.VMEM(out[3] if len(out) > 3 else out[0], out[1]) for out in sent]
        sem_count = 64
        extra = [pltpu.SMEM((BOUNDS,), jnp.int32)] if bounds else []

        def outer(*refs):
            inputs, rest = refs[: len(in_specs)], refs[len(in_specs) :]
            outputs, rest = rest[: len(out_shapes)], rest[len(out_shapes) :]
            held, rest = list(rest[: len(buffers)]), rest[len(buffers) :]
            sems, rest = rest[0], rest[1:]
            given, at, used = [], 0, 0
            for item in plan:
                if item == "f":
                    given.append(Fetch([(inputs[at], held[0])], held.pop(0), sems, used))
                    given[-1].begin()
                    used += 1
                    at += 1
                elif isinstance(item, Part):
                    buffer = held.pop(0)
                    pairs = item.copies(inputs[at : at + item.refs], buffer)
                    given.append(Fetch(pairs, buffer, sems, used))
                    if not item.late:
                        given[-1].begin()
                    used += len(pairs)
                    at += item.refs
                else:
                    given.append(inputs[at])
                    at += 1
            results = []
            for out, ref in zip(out_shapes, outputs):
                if len(out) > 2:
                    target = out[4](ref) if len(out) > 3 else ref
                    results.append(Send(held.pop(0), target, [sems.at[used], sems.at[used + 1]]))
                    used += 2
                else:
                    results.append(ref)
            assert used <= sem_count
            given = [item() if kind == "f" else item for kind, item in zip(plan, given)]
            body(*given, *results, *rest)
            for item in given:
                if isinstance(item, Fetch):
                    item()
            sends = [item for item in results if isinstance(item, Send)]
            for item in sends:
                item.finish()
            for item in sends:
                for copy in item.copies:
                    copy.wait()

        return pl.pallas_call(
            outer,
            out_shape=[jax.ShapeDtypeStruct(out[0], out[1]) for out in out_shapes],
            in_specs=in_specs,
            out_specs=[pl.BlockSpec(memory_space=pl.ANY if len(out) > 2 else pltpu.VMEM) for out in out_shapes],
            scratch_shapes=buffers
            + [pltpu.SemaphoreType.DMA((sem_count,))]
            + [pltpu.VMEM(shape, kind) for shape, kind in scratch]
            + extra,
            input_output_aliases=aliases or {},
            compiler_params=pltpu.CompilerParams(vmem_limit_bytes=megas * MEGA),
            cost_estimate=pl.CostEstimate(flops=0, bytes_accessed=0, transcendentals=0),
        )(*operands)

    return call


def fill_bounds(lengths_ref, bounds_s, total):
    bounds_s[0] = jnp.int32(0)
    end = jnp.int32(0)
    for item in range(ITEMS):
        end = end + lengths_ref[0, item]
        bounds_s[item + 1] = end
    for item in range(ITEMS + 1, BOUNDS):
        bounds_s[item] = jnp.int32(total)


def select_kernel(
    up_ref,
    up_bias_ref,
    gain_ref,
    bias_ref,
    conv_bias_ref,
    taps_ref,
    qkv_ref,
    pos_ref,
    content_ref,
    position_ref,
    up_out,
    table_out,
    qkv_out,
    pos_out,
    bias_out,
):
    place = lax.axis_index("tm")
    quarters = lax.axis_size("stream")
    share = HALF // (quarters * lax.axis_size("tm"))
    lane = lax.broadcasted_iota(jnp.int32, (1, 2 * LANES), 1)
    channel = jnp.where(lane < LANES + LOW, lane, lane - LOW)
    group = jnp.zeros_like(channel)
    for quarter in range(1, quarters):
        group = group + (channel >= quarter * share).astype(jnp.int32)
    source = group * (HALF // quarters) + share * place + channel - group * share
    chosen = (lax.broadcasted_iota(jnp.int32, (HALF, 2 * LANES), 0) == source).astype(F32).astype(BF16)
    gate = dot_nn(up_ref[:, :HALF], chosen)
    conv = dot_nn(up_ref[:, HALF:], chosen)
    up_out[:, :LANES] = gate[:, :LANES].astype(BF16)
    up_out[:, LANES : 2 * LANES] = jnp.where(low_lanes(D), gate[:, LANES:], conv[:, LANES:]).astype(BF16)
    up_out[:, 2 * LANES :] = conv[:, :LANES].astype(BF16)
    up_bias = line_of(up_bias_ref)
    lines = jnp.concatenate(
        [
            up_bias[:, :HALF],
            up_bias[:, HALF:],
            line_of(gain_ref),
            line_of(bias_ref),
            line_of(conv_bias_ref),
            jnp.zeros((3, HALF), F32),
        ],
        axis=0,
    )
    lines = dot_nn(lines.astype(BF16), chosen)
    taps = dot_nn(taps_ref[...], chosen)
    for part in range(2):
        lanes = slice(part * LANES, (part + 1) * LANES)
        table_out[part, :8] = lines[:, lanes]
        table_out[part, 8 : 8 + KERNEL] = taps[:, lanes]
        table_out[part, 8 + KERNEL :] = jnp.zeros((1, LANES), F32)

    odd = lax.rem(place, 2) == 1

    def head_lanes(ref, base):
        at = pl.ds(pl.multiple_of(lax.div(place, 2) * LANES + base, LANES), LANES)
        values = ref[:, at].astype(F32)
        values = jnp.where(odd, turn(values), values)
        return jnp.where(low_lanes(values.shape[0]), values, 0.0)

    for part in range(3):
        qkv_out[:, part * LANES : (part + 1) * LANES] = head_lanes(qkv_ref, part * D).astype(BF16)
    pos_out[...] = head_lanes(pos_ref, 0).astype(BF16)
    bias_out[...] = jnp.zeros((8, LANES), F32)
    for line, ref in enumerate((content_ref, position_ref)):
        values = line_of(ref)
        picked = values[:, :LANES]
        for tile in range(1, D // LANES):
            picked = jnp.where(
                lax.div(place, 2) == tile, values[:, tile * LANES : (tile + 1) * LANES], picked
            )
        picked = jnp.where(odd, turn(picked), picked)
        bias_out[line : line + 1] = jnp.where(low_lanes(1), picked, 0.0)


def angle_rows(coarse_ref, fine_ref, block, rows):
    half = D // 2
    base = coarse_ref[pl.ds(block, 1)]
    base_sine, base_cosine = base[:, :half], base[:, half:]
    sine, cosine = fine_ref[rows, :half], fine_ref[rows, half:]
    return base_sine * cosine + base_cosine * sine, base_cosine * cosine - base_sine * sine


def item_codes(bounds_s, index):
    code = jnp.zeros_like(index)
    for item in range(1, ITEMS + 1):
        code = code + (index >= bounds_s[item]).astype(jnp.int32)
    return jnp.where(code < ITEMS, code, ITEMS + index)


def attend_kernel(
    lengths_ref,
    x_ref,
    attn_gain_ref,
    attn_bias_ref,
    mlp_gain_ref,
    mlp_bias_ref,
    qkv_ref,
    pos_ref,
    bias_ref,
    coarse_ref,
    fine_ref,
    up_ref,
    up_bias_ref,
    n_attn_out,
    n_mlp_out,
    hat_out,
    q_position_out,
    query_out,
    key_out,
    value_out,
    prob_out,
    attn_out,
    share_out,
    stats_out,
    pre_s,
    bounds_s,
):
    frames = n_attn_out.buffer.shape[0]
    half = D // 2
    fill_bounds(lengths_ref, bounds_s, frames)
    attn_gain, attn_bias = line_of(attn_gain_ref), line_of(attn_bias_ref)
    mlp_gain, mlp_bias = line_of(mlp_gain_ref), line_of(mlp_bias_ref)
    content, position = bias_ref[0:1], bias_ref[1:2]
    x_ref = x_ref()
    begin(up_ref)

    @pl.loop(0, frames // TALL, unroll=2)
    def _(block):
        rows = rows_of(block, TALL)
        for part in range(TALL // 32):
            at = rows_of(block, TALL, part * 32)
            at = pl.ds(pl.multiple_of(block * TALL + part * 32, 32), 32)
            hat = centre_rows(x_ref[at].astype(F32))
            hat_out.buffer[at] = hat.astype(BF16)
            n_attn_out.buffer[at] = (hat * attn_gain + attn_bias).astype(BF16)
            n_mlp_out.buffer[at] = (hat * mlp_gain + mlp_bias).astype(BF16)
        parts = dot_nn(n_attn_out.buffer[rows], qkv_ref[...])
        query = parts[:, :LANES]
        query_out.buffer[rows, :LANES] = ((query + content).astype(BF16).astype(F32) * 0.125).astype(BF16)
        q_position = (query + position).astype(BF16)
        q_position_out.buffer[rows] = q_position
        key_out.buffer[rows, :LANES] = parts[:, LANES : 2 * LANES].astype(BF16)
        value_out.buffer[rows] = parts[:, 2 * LANES :].astype(BF16)
        projected = dot_nt(q_position, pos_ref[...])
        for part in range(TALL // 32):
            at = pl.ds(pl.multiple_of(block * TALL + part * 32, 32), 32)
            inner = part * 32 % BLOCK
            sine, cosine = angle_rows(
                coarse_ref, fine_ref, block * (TALL // BLOCK) + part * 32 // BLOCK, slice(inner, inner + 32)
            )
            first = projected[part * 32 : part * 32 + 32, :half]
            second = projected[part * 32 : part * 32 + 32, half:]
            query_out.buffer[at, LANES : LANES + half] = ((first * sine + second * cosine) * 0.125).astype(BF16)
            query_out.buffer[at, LANES + half :] = ((second * sine - first * cosine) * 0.125).astype(BF16)
            key_out.buffer[at, LANES : LANES + half] = cosine.astype(BF16)
            key_out.buffer[at, LANES + half :] = sine.astype(BF16)

    for out in (n_attn_out, n_mlp_out, hat_out, q_position_out, query_out, key_out, value_out):
        out.go()
    up_ref = up_ref()
    up_bias = line_of(up_bias_ref)[:, HALF:]
    lane = lax.broadcasted_iota(jnp.int32, (16, LANES), 1)

    @pl.loop(0, frames // BLOCK)
    def _(block):
        pre_s[...] = dot_nn(n_mlp_out.buffer[rows_of(block, BLOCK)], up_ref[...])
        for part in range(BLOCK // 16):
            pre = pre_s[part * 16 : part * 16 + 16] + up_bias
            hidden = pre * (0.5 + 0.5 * lax.erf(pre * math.sqrt(0.5)))
            mean = jnp.mean(hidden, axis=-1, keepdims=True)
            centred = hidden - mean
            rate = lax.rsqrt(jnp.mean(centred * centred, axis=-1, keepdims=True) + EPS)
            at = pl.ds(pl.multiple_of(block * BLOCK + part * 16, 16), 16)
            stats_out.buffer[at] = jnp.where(lane == 0, mean, rate)

    stats_out.go()
    key_code = item_codes(bounds_s, lax.broadcasted_iota(jnp.int32, (1, frames), 1))

    @pl.loop(0, frames // TALL, unroll=2)
    def _(block):
        rows = rows_of(block, TALL)
        raw = dot_nt(query_out.buffer[rows], key_out.buffer[...])
        for part in range(TALL // 32):
            start = block * TALL + part * 32
            at = pl.ds(pl.multiple_of(start, 32), 32)
            index = start + lax.broadcasted_iota(jnp.int32, (32, 1), 0)
            scaled = jnp.where(
                item_codes(bounds_s, index) == key_code, raw[part * 32 : part * 32 + 32], MASKED
            )
            weight = jnp.exp(scaled - jnp.max(scaled, axis=1, keepdims=True))
            prob_out.buffer[at] = weight.astype(BF16)
            share_out.buffer[at] = jnp.broadcast_to(1.0 / jnp.sum(weight, axis=1, keepdims=True), (32, LANES))
        attn_out.buffer[rows] = (
            dot_nn(prob_out.buffer[rows], value_out.buffer[...]) * share_out.buffer[rows]
        )


def fill_margins(wide_s, frames):
    edge = jnp.zeros((MARGIN, LANES), F32)
    wide_s[:MARGIN] = edge
    wide_s[MARGIN + frames : 2 * MARGIN + frames] = edge
    base = frames + 3 * MARGIN
    after = base + frames // 2
    low = low_lanes(MARGIN)
    wide_s[base - MARGIN : base] = jnp.where(low, 0.0, turn(wide_s[after - MARGIN : after]))
    wide_s[after : after + MARGIN] = jnp.where(low, turn(wide_s[base : base + MARGIN]), 0.0)


def item_span(bounds_s, frame):
    begin, end = bounds_s[0], bounds_s[BOUNDS - 1]
    for item in range(1, ITEMS + 1):
        edge = bounds_s[item]
        begin = jnp.where(frame >= edge, edge, begin)
    for item in range(ITEMS, 0, -1):
        edge = bounds_s[item]
        end = jnp.where(frame < edge, edge, end)
    return begin, end


def is_whole(bounds_s, start):
    begin, end = item_span(bounds_s, start)
    reach = KERNEL // 2
    low = (begin == 0) | (begin <= start - reach)
    high = (end == bounds_s[BOUNDS - 1]) | (end >= start + WINDOW + reach)
    return low & high & (end >= start + WINDOW)


def tap_limits(bounds_s, start):
    frame = start + lax.broadcasted_iota(jnp.int32, (WINDOW, LANES), 0)
    begin, end = item_span(bounds_s, frame)
    return begin - frame, end - frame


def grouped(values):
    return values.reshape(WINDOW // 8, 8, LANES)


def triple_places(step, frames):
    half = frames // 2
    return (
        pl.multiple_of(step * WINDOW, 2 * MARGIN),
        pl.multiple_of(step * WINDOW + half, 2 * MARGIN),
        pl.multiple_of(step * WINDOW + frames + 2 * MARGIN, 2 * MARGIN),
    )


def over_windows(bounds_s, frames, body):
    half = frames // 2

    @pl.loop(0, half // WINDOW)
    def _(step):
        start = step * WINDOW
        whole = is_whole(bounds_s, start) & is_whole(bounds_s, start + half)

        @pl.when(whole)
        def _():
            body(step, None)

        @pl.when(jnp.logical_not(whole))
        def _():
            first, second = tap_limits(bounds_s, start), tap_limits(bounds_s, start + half)
            low = low_lanes(WINDOW)
            rest = [jnp.where(low, one, other) for one, other in zip(first, second)]
            body(step, (first, second, rest))


def tap_view(window_ref, tap, limits):
    view = window_ref[tap + 1 : tap + 1 + WINDOW]
    if limits is not None:
        shift = tap - KERNEL // 2
        view = jnp.where((limits[0] <= shift) & (limits[1] > shift), view, 0.0)
    return grouped(view)


def mlp_first_kernel(
    lengths_ref,
    n_ref,
    up_ref,
    table_ref,
    stats_ref,
    cot_ref,
    merge_ref,
    down_ref,
    attn_ref,
    mixed_out,
    gate_pre_out,
    grad_out,
    rate_out,
    hat_out,
    early_out,
    vectors_out,
    lines_out,
    hat_s,
    slope_s,
    gate_s,
    hidden_s,
    gate_slope_s,
    conv_s,
    grad_s,
    out_s,
    back_s,
    branch_s,
    mix_s,
    taps_s,
    turn_s,
    tap_sum_s,
    columns_s,
    forward_s,
    backward_s,
    bounds_s,
):
    frames = mix_s.shape[0]
    half = frames // 2
    blocks = frames // BLOCK
    quarters, early_rows, _ = early_out.buffer.shape
    share = early_rows // 8
    channels = quarters * share
    fill_bounds(lengths_ref, bounds_s, frames)
    for part in range(2):
        for tap in range(KERNEL):
            line = jnp.broadcast_to(table_ref[part, 8 + tap : 9 + tap], (8, LANES))
            taps_s[part, tap] = line
            turn_s[part, KERNEL - 1 - tap] = line
    tap_sum_s[...] = jnp.zeros(tap_sum_s.shape, F32)
    main, rest = table_ref[0, :8], table_ref[1, :8]
    mixed_bias = jnp.where(low_lanes(1), rest[0:1], rest[1:2])
    low = low_lanes(64)
    gate_pre_ref = gate_pre_out.buffer
    n_ref = n_ref()
    stats_ref = stats_ref()
    begin(cot_ref, merge_ref, down_ref, attn_ref)

    def stat_rows(rows):
        stats = stats_ref[rows]
        return stats[:, 0:1], stats[:, 1:2]

    def chunk(start, base=0):
        return pl.ds(pl.multiple_of(start, 64) + base, 64)

    def conv_part(hidden, mean, rate, lines, rows, to_rows):
        hat = (hidden - mean) * rate
        hat_s[rows] = hat
        hat_out.buffer[rows] = hat.astype(BF16)
        conv_s[to_rows] = (hat * lines[2:3] + lines[3:4]).astype(BF16).astype(F32)

    @pl.loop(0, half // TALL)
    def _(block):
        pre = [dot_nn(n_ref[rows_of(block, TALL, base)], up_ref[...]) for base in (0, half)]
        for part in range(TALL // 64):
            inner = slice(part * 64, part * 64 + 64)
            start = block * TALL + part * 64
            mixed = []
            for values, base in zip(pre, (0, half)):
                rows = chunk(start, base)
                gate, gate_slope = gelu_parts(values[inner, :LANES] + main[0:1])
                hidden_s[rows] = gate
                gate_slope_s[rows] = gate_slope
                hidden, slope = gelu_parts(values[inner, 2 * LANES :] + main[1:2])
                mean, rate = stat_rows(rows)
                slope_s[rows] = slope * rate
                conv_part(hidden, mean, rate, main, rows, chunk(start, base + MARGIN))
                mixed.append((*gelu_parts(values[inner, LANES : 2 * LANES] + mixed_bias), mean, rate))
            (low_hidden, low_slope, low_mean, low_rate), (high_hidden, high_slope, high_mean, high_rate) = mixed
            rows = chunk(start, frames)
            hidden_s[rows] = jnp.where(low, low_hidden, turn(high_hidden))
            gate_slope_s[rows] = jnp.where(low, low_slope, turn(high_slope))
            rate = jnp.where(low, low_rate, high_rate)
            slope_s[rows] = jnp.where(low, turn(low_slope), high_slope) * rate
            conv_part(
                jnp.where(low, turn(low_hidden), high_hidden),
                jnp.where(low, low_mean, high_mean),
                rate,
                rest,
                rows,
                chunk(start, frames + 3 * MARGIN),
            )

    hat_out.go()
    fill_margins(conv_s, frames)
    tall = WINDOW + 2 * MARGIN
    outs = (0, half, frames)

    def convolve(step, limits):
        for index, base in enumerate(triple_places(step, frames)):
            forward_s[index] = conv_s[pl.ds(base, tall)]
        for index in range(3):
            own = None if limits is None else limits[index]
            total = jnp.zeros((WINDOW // 8, 8, LANES), F32)
            for tap in range(KERNEL):
                total = total + tap_view(forward_s.at[index], tap, own) * taps_s[index // 2, tap][None]
            lines = rest if index == 2 else main
            out_s[rows_of(step, WINDOW, outs[index])] = total.reshape(WINDOW, LANES) + lines[4:5]

    over_windows(bounds_s, frames, convolve)
    cot_ref = cot_ref()
    merge_ref = merge_ref()
    down_ref = down_ref()
    attn_ref = attn_ref()
    down_ref[channels:] = jnp.zeros((2 * LANES - channels, D), BF16)
    zero = jnp.zeros((8, LANES), F32)

    def branch_part(grad_gated, rows, to_rows, sums):
        up_sum, conv_sum = sums
        gate, conv = hidden_s[rows], out_s[rows]
        gate_pre = (grad_gated * conv * gate_slope_s[rows]).astype(BF16)
        gate_pre_ref[rows] = gate_pre
        grad_conv = (grad_gated * gate).astype(BF16).astype(F32)
        grad_s[to_rows] = grad_conv
        gate_pre = gate_pre.astype(F32)
        return gate * conv, gate_pre, (up_sum + fold_rows(gate_pre), conv_sum + fold_rows(grad_conv))

    def branch_step(block, sums):
        main_sums, rest_sums = sums
        grads = []
        for base in (0, half):
            rows = rows_of(block, TALL, base)
            branch = dot_nt(cot_ref[rows], merge_ref[...]).astype(BF16)
            branch_s[rows] = branch
            grads.append(dot_nt(branch, down_ref[...]))
        for part in range(TALL // 64):
            inner = slice(part * 64, part * 64 + 64)
            start = block * TALL + part * 64
            for values, base in zip(grads, (0, half)):
                rows = chunk(start, base)
                gated, gate_pre, main_sums = branch_part(
                    values[inner, :LANES], rows, chunk(start, base + MARGIN), main_sums
                )
                mix_s[rows, :LANES] = gated.astype(BF16)
                gate_s[rows, :LANES] = gate_pre.astype(BF16)
            grad = jnp.where(low, grads[0][inner, LANES:], turn(grads[1][inner, LANES:]))
            gated, gate_pre, rest_sums = branch_part(
                grad, chunk(start, frames), chunk(start, frames + 3 * MARGIN), rest_sums
            )
            low_rows, high_rows = chunk(start), chunk(start, half)
            gate_s[low_rows, LANES:] = gate_pre.astype(BF16)
            gate_s[high_rows, LANES:] = turn(gate_pre).astype(BF16)
            mix_s[low_rows, LANES:] = jnp.where(low, gated, turn(attn_ref[low_rows])).astype(BF16)
            mix_s[high_rows, LANES:] = jnp.where(low, turn(gated), turn(attn_ref[high_rows])).astype(BF16)
        return main_sums, rest_sums

    (main_up, main_conv), (rest_up, rest_conv) = lax.fori_loop(
        0, half // TALL, branch_step, ((zero, zero), (zero, zero))
    )
    gate_pre_out.go()
    fill_margins(grad_s, frames)
    ones = jnp.ones((16, frames), BF16)
    lines_out[0:1] = dot_nn(ones, branch_s[...])[0:1]
    lines_out[1:2] = dot_nn(ones, cot_ref[...])[0:1]
    lines_out[2:8] = jnp.zeros((6, D), F32)
    grad_down = dot_tn(mix_s[...], branch_s[...])
    grad_gate = dot_tn(gate_s[...], n_ref[...])
    for quarter in range(quarters):
        for tile in range(4):
            early_out.buffer[quarter, tile * share : (tile + 1) * share] = grad_down[
                quarter * share : (quarter + 1) * share, tile * LANES : (tile + 1) * LANES
            ].astype(BF16)
        early_out.buffer[quarter, 4 * share :] = grad_gate[
            :channels, quarter * LANES : (quarter + 1) * LANES
        ].astype(BF16)
    early_out.go()
    for block in range(blocks):
        mixed_out.buffer[block, :BLOCK] = mix_s[block * BLOCK : (block + 1) * BLOCK]
    mixed_out.go(slice(None), pl.ds(0, BLOCK))

    def differentiate(step, limits):
        for index, base in enumerate(triple_places(step, frames)):
            forward_s[index] = conv_s[pl.ds(base, tall)]
            backward_s[index] = grad_s[pl.ds(base, tall)]
        for index in range(3):
            own = None if limits is None else limits[index]
            total = jnp.zeros((WINDOW // 8, 8, LANES), F32)
            centre = grouped(backward_s[index, MARGIN : MARGIN + WINDOW])
            for tap in range(KERNEL):
                total = total + tap_view(backward_s.at[index], tap, own) * turn_s[index // 2, tap][None]
                tap_sum_s[index // 2, tap] += jnp.sum(tap_view(forward_s.at[index], tap, own) * centre, axis=0)
            back_s[rows_of(step, WINDOW, outs[index])] = total.reshape(WINDOW, LANES)

    over_windows(bounds_s, frames, differentiate)
    lane = lax.broadcasted_iota(jnp.int32, (64, LANES), 1)

    def norm_part(rows, lines, sums):
        gain_sum, bias_sum = sums
        back, hat, slope = back_s[rows], hat_s[rows], slope_s[rows]
        grad = back * lines[2:3]
        grad_out.buffer[rows] = (grad * slope).astype(BF16)
        rate_out.buffer[rows] = slope.astype(BF16)
        along = back * hat
        return grad, along * lines[2:3], (gain_sum + fold_rows(along), bias_sum + fold_rows(back))

    def norm_step(block, sums):
        main_sums, rest_sums = sums
        for part in range(TALL // 64):
            start = block * TALL + part * 64
            pairs = []
            for base in (0, half):
                plain, along, main_sums = norm_part(chunk(start, base), main, main_sums)
                pairs.append([plain, along])
            plain, along, rest_sums = norm_part(chunk(start, frames), rest, rest_sums)
            for item, values in enumerate((plain, along)):
                pairs[0][item] = pairs[0][item] + jnp.where(low, values, 0.0)
                pairs[1][item] = pairs[1][item] + jnp.where(low, 0.0, values)
            for (plain, along), base in zip(pairs, (0, half)):
                columns_s[chunk(start, base)] = jnp.where(
                    lane == 0,
                    jnp.sum(plain, axis=-1, keepdims=True),
                    jnp.where(lane == 1, jnp.sum(along, axis=-1, keepdims=True), 0.0),
                )
        return main_sums, rest_sums

    (main_gain, main_bias), (rest_gain, rest_bias) = lax.fori_loop(
        0, half // TALL, norm_step, ((zero, zero), (zero, zero))
    )
    grad_out.go()
    rate_out.go()
    totals = jnp.concatenate(
        [jnp.transpose(columns_s[block * BLOCK : (block + 1) * BLOCK])[:2] for block in range(blocks)], axis=0
    )
    high = totals.astype(BF16)
    low_part = (totals - high.astype(F32)).astype(BF16)
    for block in range(blocks):
        mixed_out.buffer[block, BLOCK:, :LANES] = high
        mixed_out.buffer[block, BLOCK:, LANES:] = low_part
    mixed_out.go(slice(None), pl.ds(BLOCK, 2 * blocks))

    def vectors(part, lines):
        taps = jnp.sum(tap_sum_s[part], axis=1)[:KERNEL]
        stacked = jnp.concatenate([taps] + [one_row(line) for line in lines], axis=0)
        if part:
            stacked = stacked + turn(stacked)
        return jnp.transpose(
            jnp.concatenate([stacked, jnp.zeros((LANES - stacked.shape[0], LANES), F32)], axis=0)
        )

    vectors_out[:LANES] = vectors(0, (main_conv, main_gain, main_bias, main_up))
    vectors_out[LANES:] = vectors(1, (rest_conv, rest_gain, rest_bias, rest_up))[: channels - LANES]


def attend_back_kernel(
    cot_ref,
    merge_ref,
    head_ref,
    share_ref,
    value_ref,
    attn_ref,
    prob_ref,
    key_ref,
    coarse_ref,
    fine_ref,
    pos_ref,
    query_ref,
    n_ref,
    q_position_ref,
    qkv_ref,
    hat_ref,
    gain_ref,
    early_ref,
    branch_out,
    total_out,
    pack_0,
    pack_1,
    pack_2,
    pack_3,
    lines_out,
    grad_s,
    raw_s,
    projected_s,
    parts_s,
    grads_s,
):
    place = lax.axis_index("tm")
    frames = raw_s.shape[0]
    blocks = frames // BLOCK
    half = D // 2
    zero = jnp.zeros((8, LANES), F32)
    cot_ref, merge_ref, head_ref, share_ref = cot_ref(), merge_ref(), head_ref(), share_ref()
    head_ref[HEAD:] = jnp.zeros((LANES - HEAD, D), BF16)
    begin(value_ref, attn_ref, prob_ref, key_ref, pos_ref)

    @pl.loop(0, frames // TALL, unroll=2)
    def _(block):
        rows = rows_of(block, TALL)
        branch = dot_nt(cot_ref[rows], merge_ref[...]).astype(BF16)
        branch_out.buffer[rows] = branch
        grad_s[rows] = (dot_nt(branch, head_ref[...]) * share_ref[rows]).astype(BF16)

    branch_out.go()
    value_ref, attn_ref, prob_ref = value_ref(), attn_ref(), prob_ref()
    key_ref, pos_ref = key_ref(), pos_ref()
    begin(query_ref, n_ref, q_position_ref, qkv_ref, hat_ref, early_ref)

    def score_step(block, sums):
        content_sum, position_sum = sums
        rows = rows_of(block, TALL)
        grad = grad_s[rows]
        score = dot_nt(grad, value_ref[...])
        for part in range(TALL // 32):
            at = pl.ds(pl.multiple_of(block * TALL + part * 32, 32), 32)
            inner = slice(part * 32, part * 32 + 32)
            delta = jnp.sum(grad[inner].astype(F32) * attn_ref[at], axis=1, keepdims=True)
            raw_s[at] = (prob_ref[at].astype(F32) * (score[inner] - delta)).astype(BF16)
        query = dot_nn(raw_s[rows], key_ref[...]) * 0.125
        for part in range(TALL // 32):
            at = pl.ds(pl.multiple_of(block * TALL + part * 32, 32), 32)
            inner = part * 32 % BLOCK
            sine, cosine = angle_rows(
                coarse_ref, fine_ref, block * (TALL // BLOCK) + part * 32 // BLOCK, slice(inner, inner + 32)
            )
            inner = slice(part * 32, part * 32 + 32)
            first, second = query[inner, LANES : LANES + half], query[inner, LANES + half :]
            projected_s[at, :half] = (first * sine - second * cosine).astype(BF16)
            projected_s[at, half:] = (first * cosine + second * sine).astype(BF16)
        position = dot_nn(projected_s[rows], pos_ref[...])
        content = query[:, :LANES]
        parts_s[rows, :LANES] = (content + position).astype(BF16)
        return content_sum + fold_rows(content), position_sum + fold_rows(position)

    content_sum, position_sum = lax.fori_loop(0, frames // TALL, score_step, (zero, zero), unroll=2)
    query_ref, n_ref, q_position_ref = query_ref(), n_ref(), q_position_ref()
    qkv_ref, hat_ref = qkv_ref(), hat_ref()
    grad_key = dot_tn(query_ref[...], raw_s[...])
    grad_value = dot_tn(grad_s[...], prob_ref[...])
    for block in range(blocks):
        at = slice(block * BLOCK, (block + 1) * BLOCK)
        parts_s[at, LANES : 2 * LANES] = jnp.transpose(grad_key[:, at]).astype(BF16)
        parts_s[at, 2 * LANES :] = jnp.transpose(grad_value[:, at]).astype(BF16)
    grads_s[:HEAD] = dot_tn(parts_s[:, :LANES], n_ref[...])[:HEAD]
    grads_s[HEAD : 2 * HEAD] = dot_nn(grad_key.astype(BF16), n_ref[...])[:HEAD]
    grads_s[2 * HEAD : 3 * HEAD] = dot_nn(grad_value.astype(BF16), n_ref[...])[:HEAD]
    grads_s[3 * HEAD :] = dot_tn(q_position_ref[...], projected_s[...])[:HEAD]
    stream = lax.axis_index("stream")
    early_ref = early_ref()
    for apart, pack_out in enumerate((pack_0, pack_1, pack_2, pack_3)):
        quarter = lax.bitwise_xor(stream, jnp.int32(apart))
        lanes = pl.ds(pl.multiple_of(quarter * LANES, LANES), LANES)
        pack_out.buffer[: 4 * HEAD] = grads_s[:, lanes].astype(BF16)
        pack_out.buffer[4 * HEAD :] = early_ref[quarter]
        pack_out.go()
    gain = line_of(gain_ref)
    wide_zero = jnp.zeros((8, D), F32)

    def norm_step(block, sums):
        gain_sum, bias_sum = sums
        grad = dot_nt(parts_s[rows_of(block, TALL)], qkv_ref[...])
        for part in range(TALL // 32):
            at = pl.ds(pl.multiple_of(block * TALL + part * 32, 32), 32)
            own = grad[part * 32 : part * 32 + 32]
            total_out.buffer[at] = (own * gain).astype(BF16)
            gain_sum = gain_sum + fold_rows(own * hat_ref[at].astype(F32))
            bias_sum = bias_sum + fold_rows(own)
        return gain_sum, bias_sum

    gain_sum, bias_sum = lax.fori_loop(0, frames // TALL, norm_step, (wide_zero, wide_zero), unroll=2)
    lane = lax.broadcasted_iota(jnp.int32, (1, LANES), 1)

    def own_lanes(sums):
        line = one_row(sums)
        line = line + turn(line)
        tiles = [
            jnp.where(lax.div(tile * LANES + lane, HEAD) == place, line, 0.0) for tile in range(D // LANES)
        ]
        return jnp.concatenate(tiles, axis=1)

    lines_out[...] = jnp.concatenate(
        [
            one_row(gain_sum),
            one_row(bias_sum),
            own_lanes(content_sum),
            own_lanes(position_sum),
            jnp.zeros((4, D), F32),
        ],
        axis=0,
    )


def mlp_second_kernel(
    mixed_ref,
    gate_pre_ref,
    grad_ref,
    rate_ref,
    hat_ref,
    up_ref,
    norm_hat_ref,
    gain_ref,
    other_ref,
    n_ref,
    vectors_ref,
    first_lines_ref,
    head_lines_ref,
    total_out,
    pack_0,
    pack_1,
    pack_2,
    pack_3,
    pre_s,
    columns_s,
    grad_up_s,
    lines_s,
    up_columns_s,
):
    packs = (pack_0, pack_1, pack_2, pack_3)
    stream = lax.axis_index("stream")
    place = lax.axis_index("tm")
    frames = pre_s.shape[0]
    half = frames // 2
    blocks = frames // BLOCK
    quarters = len(packs)
    channels = vectors_ref.shape[0]
    share = channels // quarters
    totals = jnp.zeros((2 * blocks, LANES), F32)
    mixed_ref = mixed_ref()
    for source in range(mixed_ref.shape[0]):
        both = mixed_ref[source].astype(F32)
        totals = totals + (both[:, :LANES] + both[:, LANES:])
    totals = totals * (1.0 / HALF)
    columns = jnp.transpose(jnp.concatenate([totals, jnp.zeros((LANES - 2 * blocks, LANES), F32)], axis=0))
    lane = lax.broadcasted_iota(jnp.int32, (BLOCK, LANES), 1)
    for block in range(blocks):
        columns_s[block * BLOCK : (block + 1) * BLOCK] = jnp.where(
            lane == 0, columns[:, 2 * block : 2 * block + 1], columns[:, 2 * block + 1 : 2 * block + 2]
        )
    gate_pre_ref, grad_ref, rate_ref, hat_ref = gate_pre_ref(), grad_ref(), rate_ref(), hat_ref()
    begin(n_ref, up_ref, norm_hat_ref, other_ref)
    low = low_lanes(64)
    gain = line_of(gain_ref)

    def chunk(start, base=0):
        return pl.ds(pl.multiple_of(start, 64) + base, 64)

    def pre_part(rows, table, up_sum):
        plain, along = table
        hat, rate = hat_ref[rows].astype(F32), rate_ref[rows].astype(F32)
        pre = (grad_ref[rows].astype(F32) - rate * (plain + hat * along)).astype(BF16).astype(F32)
        return pre, up_sum + fold_rows(pre)

    def pre_step(block, sums):
        main_up, rest_up = sums
        for part in range(TALL // 64):
            start = block * TALL + part * 64
            tables = []
            for base in (0, half):
                rows = chunk(start, base)
                values = columns_s[rows]
                table = [values[:, item : item + 1] for item in range(2)]
                tables.append(table)
                pre, main_up = pre_part(rows, table, main_up)
                pre_s[rows, :LANES] = gate_pre_ref[rows]
                pre_s[rows, 2 * LANES :] = pre.astype(BF16)
            rows = chunk(start, frames)
            table = [jnp.where(low, one, other) for one, other in zip(*tables)]
            pre, rest_up = pre_part(rows, table, rest_up)
            gate_pre = gate_pre_ref[rows].astype(F32)
            pre_s[chunk(start), LANES : 2 * LANES] = jnp.where(low, gate_pre, turn(pre)).astype(BF16)
            pre_s[chunk(start, half), LANES : 2 * LANES] = jnp.where(low, turn(gate_pre), pre).astype(BF16)
        return main_up, rest_up

    zero = jnp.zeros((8, LANES), F32)
    main_up, rest_up = lax.fori_loop(0, half // TALL, pre_step, (zero, zero))
    n_ref, up_ref, norm_hat_ref, other_ref = n_ref(), up_ref(), norm_hat_ref(), other_ref()
    grad_up_s[...] = dot_tn(pre_s[:, LANES:], n_ref[...])
    wide_zero = jnp.zeros((8, D), F32)

    def norm_step(block, sums):
        gain_sum, bias_sum = sums
        rows = rows_of(block, BLOCK)
        grad = dot_nt(pre_s[rows], up_ref[...])
        total_out.buffer[block] = (grad * gain + other_ref[rows].astype(F32)).astype(BF16)
        return gain_sum + fold_rows(grad * norm_hat_ref[rows].astype(F32)), bias_sum + fold_rows(grad)

    gain_sum, bias_sum = lax.fori_loop(0, blocks, norm_step, (wide_zero, wide_zero), unroll=2)
    total_out.go()
    rest_line = one_row(rest_up)
    up_columns_s[:LANES] = jnp.transpose(jnp.broadcast_to(one_row(main_up), (LANES, LANES)))
    up_columns_s[LANES:] = jnp.transpose(jnp.broadcast_to(rest_line + turn(rest_line), (LANES, LANES)))[:LOW]
    first_device = (place == 0).astype(F32)
    lines_s[...] = jnp.concatenate(
        [
            head_lines_ref[0:2],
            one_row(gain_sum),
            one_row(bias_sum),
            head_lines_ref[2:4],
            first_lines_ref[0:2] * first_device,
            jnp.zeros((8, D), F32),
        ],
        axis=0,
    )
    gate_at = KERNEL + 3
    lane = lax.broadcasted_iota(jnp.int32, (share, LANES), 1)
    for apart, pack_out in enumerate(packs):
        quarter = lax.bitwise_xor(stream, jnp.int32(apart))
        lanes = pl.ds(pl.multiple_of(quarter * LANES, LANES), LANES)
        pack_out[:LANES] = grad_up_s[LANES:, lanes].astype(BF16)
        pack_out[LANES:channels] = grad_up_s[LOW:LANES, lanes].astype(BF16)
        table = vectors_ref[pl.ds(pl.multiple_of(quarter * share, 8), share)]
        for other in range(2):
            at = pl.ds(pl.multiple_of((2 * lax.rem(quarter, 2) + other) * share, 8), share)
            column = jnp.where(
                quarter < quarters // 2, vectors_ref[at][:, gate_at : gate_at + 1], up_columns_s[at][:, 0:1]
            )
            table = jnp.where(lane == gate_at + other, column, table)
        pack_out[channels : channels + share] = table.astype(BF16)
        pack_out[channels + share :] = lines_s[:, lanes].astype(BF16)


def output_kernel(
    x_ref, mixed_ref, head_ref, down_ref, down_bias_ref, merge_ref, merge_bias_ref, out_ref, joined_out
):
    sources = mixed_ref.shape[0]
    rows = x_ref.shape[0]
    channels = HALF // sources
    share = channels // 4
    attn_parts = []
    branch_attn = jnp.zeros((rows, D), F32)
    branch_mlp = jnp.zeros((rows, D), F32)
    for source in range(sources):
        attn = turn(mixed_ref[source, :rows, LANES:].astype(F32))[:, :HEAD].astype(BF16)
        attn_parts.append(attn)
        branch_attn = branch_attn + dot_nn(attn, head_ref[source * HEAD : (source + 1) * HEAD])
        down = jnp.concatenate(
            [down_ref[(part * sources + source) * share : (part * sources + source + 1) * share] for part in range(4)],
            axis=0,
        )
        branch_mlp = branch_mlp + dot_nn(mixed_ref[source, :rows, :channels], down)
    joined = jnp.concatenate(
        [branch_attn.astype(BF16), (branch_mlp + line_of(down_bias_ref)).astype(BF16)], axis=1
    )
    result = x_ref[...].astype(F32) + dot_nn(joined, merge_ref[...]) + line_of(merge_bias_ref)
    out_ref[...] = result.astype(BF16)
    turned = jnp.transpose(joined.astype(F32))
    heads = jnp.transpose(jnp.concatenate(attn_parts, axis=1).astype(F32))
    merge_share = turned.shape[0] // (4 * sources)
    head_share = heads.shape[0] // (4 * sources)
    used = 4 * (merge_share + head_share)
    for target in range(sources):
        for part in range(4):
            at = (part * sources + target) * merge_share
            joined_out[target, part * merge_share : (part + 1) * merge_share] = turned[
                at : at + merge_share
            ].astype(BF16)
            at = (part * sources + target) * head_share
            to = 4 * merge_share + part * head_share
            joined_out[target, to : to + head_share] = heads[at : at + head_share].astype(BF16)
        joined_out[target, used:] = jnp.zeros((joined_out.shape[1] - used, rows), BF16)


def merge_kernel(joined_ref, branch_ref, cot_ref, up_0, up_1, up_2, up_3, pack_0, pack_1, pack_2, pack_3, merge_s, head_s):
    stream = lax.axis_index("stream")
    cot_ref = cot_ref()
    sources, _, rows = joined_ref.shape
    merge_rows = 2 * D // sources
    head_rows = D // sources
    grad_merge = jnp.zeros((merge_rows, D), F32)
    grad_head = jnp.zeros((head_rows, D), F32)
    for source in range(sources):
        at = slice(source * rows, (source + 1) * rows)
        joined = joined_ref[source]
        grad_merge = grad_merge + dot_nn(joined[:merge_rows], cot_ref[at])
        grad_head = grad_head + dot_nn(joined[merge_rows : merge_rows + head_rows], branch_ref[at])
    merge_s[...] = grad_merge
    head_s[...] = grad_head
    first = up_0.shape[0]
    ups = (up_0, up_1, up_2, up_3)
    for apart, pack_out in enumerate((pack_0, pack_1, pack_2, pack_3)):
        pack_out = pack_out.buffer
        pack_out[:first] = ups[apart][...]
        quarter = lax.bitwise_xor(stream, jnp.int32(apart))
        for grad_s, base in ((merge_s, first), (head_s, first + merge_rows)):
            share = grad_s.shape[0] // 4
            at = pl.ds(pl.multiple_of(quarter * share, share), share)
            for tile in range(4):
                to = base + tile * share
                pack_out[to : to + share] = grad_s[at, tile * LANES : (tile + 1) * LANES].astype(BF16)


def frames_kernel(x_ref, cot_ref, total_ref, out_ref):
    for part in range(x_ref.shape[0] // 32):
        rows = slice(part * 32, part * 32 + 32)
        inputs = x_ref[rows].astype(F32)
        mean = jnp.mean(inputs, axis=-1, keepdims=True)
        centred = inputs - mean
        rate = lax.rsqrt(jnp.mean(centred * centred, axis=-1, keepdims=True) + EPS)
        hat = centred * rate
        grad = total_ref[0, rows].astype(F32)
        for source in range(1, total_ref.shape[0]):
            grad = grad + total_ref[source, rows].astype(F32)
        plain = jnp.mean(grad, axis=-1, keepdims=True)
        along = jnp.mean(grad * hat, axis=-1, keepdims=True)
        out_ref[rows] = cot_ref[rows].astype(F32) + rate * (grad - plain - hat * along)


def add_kernel(*refs):
    out_ref = refs[-1]
    first = 0
    for at in range(0, len(refs) - 1, 4):
        total = refs[at][...].astype(F32)
        for ref in refs[at + 1 : at + 4]:
            total = total + ref[...].astype(F32)
        out_ref[first : first + total.shape[0]] = total.astype(BF16)
        first += total.shape[0]


def gather_parts(part_refs, all_s):
    place = lax.axis_index("tm")
    for apart, part_ref in enumerate(part_refs):
        all_s[lax.bitwise_xor(jnp.int32(apart), place)] = part_ref[...]


def lines_from(all_s, base, size):
    return jnp.concatenate([all_s[source, base : base + size] for source in range(all_s.shape[0])], axis=0).astype(F32)


def early_kernel(*refs):
    qkv_out, pos_out, down_out, up_out, all_s = refs[HEADS:]
    gather_parts(refs[:HEADS], all_s)
    sources = all_s.shape[0]
    share = HALF // (4 * sources)
    for kind in range(4):
        lines = jnp.transpose(lines_from(all_s, kind * HEAD, HEAD))
        if kind < 3:
            qkv_out[:, kind * D : (kind + 1) * D] = lines
        else:
            pos_out[...] = lines
    base = 4 * HEAD
    for source in range(sources):
        for tile in range(4):
            down_out[source * share : (source + 1) * share, tile * LANES : (tile + 1) * LANES] = all_s[
                source, base + tile * share : base + (tile + 1) * share
            ].astype(F32)
    wide = sources * share
    for group in range(4):
        up_out.buffer[:, group * wide : (group + 1) * wide] = jnp.transpose(
            lines_from(all_s, base + 4 * share + group * share, share)
        )


def late_kernel(*refs):
    part_refs = refs[1 : HEADS + 1]
    (
        attn_gain_out,
        attn_bias_out,
        mlp_gain_out,
        mlp_bias_out,
        content_out,
        position_out,
        outw_out,
        up_out,
        up_bias_out,
        gain_out,
        bias_out,
        taps_out,
        conv_bias_out,
        down_bias_out,
        merge_out,
        merge_bias_out,
        all_s,
    ) = refs[HEADS + 1 :]
    gather_parts(part_refs, all_s)
    sources = all_s.shape[0]
    channels = HALF // sources
    share = channels // 4
    base = 0
    for group in range(4):
        at = group * sources * share
        up_out.buffer[:, at : at + sources * share] = jnp.transpose(lines_from(all_s, base + group * share, share))
    up_out.go()
    table = jnp.transpose(lines_from(all_s, base + channels, share))
    taps_out[...] = table[:KERNEL]
    conv_bias_out[...] = table[KERNEL]
    gain_out[...] = table[KERNEL + 1]
    bias_out[...] = table[KERNEL + 2]
    wide = sources * share
    up_bias_out[:wide] = table[KERNEL + 3]
    up_bias_out[wide:] = table[KERNEL + 4]
    base = base + channels + share
    lines = all_s[0, base : base + 16].astype(F32)
    for source in range(1, sources):
        lines = lines + all_s[source, base : base + 16].astype(F32)
    outs = (attn_gain_out, attn_bias_out, mlp_gain_out, mlp_bias_out, content_out, position_out, down_bias_out, merge_bias_out)
    for line, out in enumerate(outs):
        out[...] = lines[line]
    base = base + 16
    merge_share = 2 * D // (4 * sources)
    head_share = D // (4 * sources)
    for source in range(sources):
        for tile in range(4):
            lanes = slice(tile * LANES, (tile + 1) * LANES)
            at = base + tile * merge_share
            merge_out[source * merge_share : (source + 1) * merge_share, lanes] = all_s[
                source, at : at + merge_share
            ].astype(F32)
            at = base + 4 * merge_share + tile * head_share
            outw_out[source * head_share : (source + 1) * head_share, lanes] = all_s[
                source, at : at + head_share
            ].astype(F32)


def moved(block, axis, bits):
    count = lax.axis_size(axis)
    return lax.ppermute(block, axis, [(index, index ^ bits) for index in range(count)])


def over_streams(packs):
    return [packs[0]] + [moved(packs[bits], "stream", bits) for bits in range(1, lax.axis_size("stream"))]


def near_blocks(block):
    return [block] + [moved(block, "tm", bits) for bits in range(2, lax.axis_size("tm"), 2)]


def far_blocks(near):
    far = [moved(part, "tm", 1) for part in near]
    return [part for pair in zip(near, far) for part in pair]


def spread(block):
    return far_blocks(near_blocks(block))


def head_device(
    frames,
    lengths,
    cotangent,
    ln_attn_gain,
    ln_attn_bias,
    ln_mlp_gain,
    ln_mlp_bias,
    qkv_weight,
    content_bias,
    position_bias,
    pos_weight,
    out_weight,
    up_weight,
    up_bias,
    gate_norm_gain,
    gate_norm_bias,
    conv_kernel,
    conv_bias,
    down_weight,
    down_bias,
    merge_weight,
    merge_bias,
):
    count = lax.axis_size("tm")
    quarters = lax.axis_size("stream")
    own = frames.shape[1]
    total = own * count
    folded = total + total // 2
    padded = folded + 4 * MARGIN
    share = HALF // (quarters * count)
    channels = HALF // count
    quarter = D // quarters
    own_frames = frames[0]
    own_cotangent = cotangent[0]

    whole, late = Part(), Part(late=True)
    near = near_blocks(own_frames)
    cot_near = near_blocks(own_cotangent)
    up_own, table, qkv_own, pos_own, bias_own = kernel_call(
        select_kernel,
        [
            ((D, 3 * LANES), BF16),
            ((2, 8 + KERNEL + 1, LANES), F32),
            ((D, 3 * LANES), BF16),
            ((D, LANES), BF16),
            ((8, LANES), F32),
        ],
        10 * "v",
    )(
        up_weight,
        up_bias,
        gate_norm_gain,
        gate_norm_bias,
        conv_bias,
        conv_kernel,
        qkv_weight,
        pos_weight,
        content_bias,
        position_bias,
    )
    near, up_own = lax.optimization_barrier((near, up_own))
    blocks = far_blocks(near)
    frequency = jnp.exp(jnp.arange(D // 2, dtype=F32) * (-2.0 * math.log(10000.0) / D))
    coarse = jnp.arange(0, total, BLOCK, dtype=F32)[:, None] * frequency[None]
    fine = jnp.arange(BLOCK, dtype=F32)[:, None] * frequency[None]
    coarse_table = jnp.concatenate([jnp.sin(coarse), jnp.cos(coarse)], axis=1)
    fine_table = jnp.concatenate([jnp.sin(fine), jnp.cos(fine)], axis=1)

    n_attn, n_mlp, hat, q_position, query, key, value, prob, attn, row_share, stats = kernel_call(
        attend_kernel,
        [
            ((total, D), BF16, 1),
            ((total, D), BF16, 1),
            ((total, D), BF16, 1),
            ((total, LANES), BF16, 1),
            ((total, LANES + D), BF16, 1),
            ((total, LANES + D), BF16, 1),
            ((total, LANES), BF16, 1),
            ((total, total), BF16, 1),
            ((total, LANES), F32, 1),
            ((total, LANES), F32, 1),
            ((total, LANES), F32, 1),
        ],
        [
            "s",
            blocks_part(),
            *"vvvvvvvvv",
            Part((D, HALF), lambda refs, buffer: [(refs[0].at[:, pl.ds(HALF, HALF)], buffer)], late=True),
            "v",
        ],
        [((BLOCK, HALF), F32)],
        bounds=True,
    )(
        lengths,
        *blocks,
        ln_attn_gain,
        ln_attn_bias,
        ln_mlp_gain,
        ln_mlp_bias,
        qkv_own,
        pos_own,
        bias_own,
        coarse_table,
        fine_table,
        up_weight,
        up_bias,
    )

    n_mlp, cot_near = lax.optimization_barrier((n_mlp, cot_near))
    cot = far_blocks(cot_near)

    def own_down(refs, buffer):
        place = lax.axis_index("tm")
        stride = HALF // quarters
        return [
            (
                refs[0].at[pl.ds(pl.multiple_of(part * stride + share * place, 16), share)],
                buffer.at[pl.ds(part * share, share)],
            )
            for part in range(quarters)
        ]

    mixed, gate_pre, grad_y, slope, gate_hat, early_pack, vectors, first_lines = kernel_call(
        mlp_first_kernel,
        [
            ((count, own + 16, 2 * LANES), BF16, 1),
            ((folded, LANES), BF16, 1),
            ((folded, LANES), BF16, 1),
            ((folded, LANES), BF16, 1),
            ((folded, LANES), BF16, 1),
            ((quarters, 8 * share, LANES), BF16, 1),
            ((channels, LANES), F32),
            ((8, D), F32),
        ],
        [
            "s",
            whole,
            "v",
            "v",
            whole,
            blocks_part(late=True),
            rows_part(D, D, late=True),
            Part((2 * LANES, D), own_down, late=True),
            Part(late=True),
        ],
        [
            ((folded, LANES), F32),
            ((folded, LANES), F32),
            ((total, 2 * LANES), BF16),
            ((folded, LANES), F32),
            ((folded, LANES), F32),
            ((padded, LANES), F32),
            ((padded, LANES), F32),
            ((folded, LANES), F32),
            ((folded, LANES), F32),
            ((total, D), BF16),
            ((total, 2 * LANES), BF16),
            ((2, 32, 8, LANES), F32),
            ((2, 32, 8, LANES), F32),
            ((2, 32, 8, LANES), F32),
            ((total, LANES), F32),
            ((3, WINDOW + 2 * MARGIN, LANES), F32),
            ((3, WINDOW + 2 * MARGIN, LANES), F32),
        ],
        bounds=True,
    )(lengths, n_mlp, up_own, table, stats, *cot, merge_weight, down_weight, attn)
    mixed_own = lax.all_to_all(mixed, "tm", 0, 0, tiled=True)

    def own_head(refs, buffer):
        at = pl.ds(pl.multiple_of(lax.axis_index("tm") * HEAD, HEAD), HEAD)
        return [(refs[0].at[at], buffer.at[pl.ds(0, HEAD)])]

    branch, from_attn, *head_packs, head_lines = kernel_call(
        attend_back_kernel,
        [
            ((total, D), BF16, 1),
            ((total, D), BF16, 1),
            *([((4 * HEAD + 8 * share, LANES), BF16, 1)] * quarters),
            ((8, D), F32),
        ],
        [
            blocks_part(),
            rows_part(0, D),
            Part((LANES, D), own_head),
            whole,
            late,
            late,
            late,
            late,
            "v",
            "v",
            late,
            Part((total, LANES), lambda refs, buffer: [(refs[0].at[:, pl.ds(0, LANES)], buffer)], late=True),
            late,
            late,
            late,
            late,
            "v",
            late,
        ],
        [
            ((total, LANES), BF16),
            ((total, total), BF16),
            ((total, D), BF16),
            ((total, 3 * LANES), BF16),
            ((4 * HEAD, D), F32),
        ],
    )(
        *cot,
        merge_weight,
        out_weight,
        row_share,
        value,
        attn,
        prob,
        key,
        coarse_table,
        fine_table,
        pos_own,
        query,
        n_attn,
        q_position,
        qkv_own,
        hat,
        ln_attn_gain,
        early_pack,
    )
    head_parts = over_streams(head_packs)
    mixed_own, _ = lax.optimization_barrier((mixed_own, head_lines))
    out_rows, joined = kernel_call(
        output_kernel,
        [((own, D), BF16), ((count, 256, own), BF16)],
        "vvvvvvv",
        megas=24,
    )(own_frames, mixed_own, out_weight, down_weight, down_bias, merge_weight, merge_bias)
    joined_all = lax.all_to_all(joined, "tm", 0, 0, tiled=True)
    gate_pre, _ = lax.optimization_barrier((gate_pre, joined))
    up_rows = 5 * share + 16
    from_both, *up_packs = kernel_call(
        mlp_second_kernel,
        [((count, own, D), BF16, 1)] + [((up_rows, LANES), BF16)] * quarters,
        [
            Part(
                (count, 2 * total // BLOCK, 2 * LANES),
                lambda refs, buffer: [(refs[0].at[:, pl.ds(own, 2 * total // BLOCK)], buffer)],
            ),
            *([whole] * 4),
            late,
            late,
            "v",
            late,
            late,
            *"vvv",
        ],
        [
            ((total, 3 * LANES), BF16),
            ((total, LANES), F32),
            ((2 * LANES, D), F32),
            ((16, D), F32),
            ((channels, LANES), F32),
        ],
    )(
        mixed_own,
        gate_pre,
        grad_y,
        slope,
        gate_hat,
        up_own,
        hat,
        ln_mlp_gain,
        from_attn,
        n_mlp,
        vectors,
        first_lines,
        head_lines,
    )
    joined_all, up_packs, head_parts, from_both = lax.optimization_barrier(
        (joined_all, up_packs, head_parts, from_both)
    )
    from_all = lax.all_to_all(from_both, "tm", 0, 0, tiled=True)
    late_rows = up_rows + 3 * D // count
    late_packs = kernel_call(
        merge_kernel,
        [((late_rows, LANES), BF16, 1)] * quarters,
        ["f", "f", blocks_part(), *"ffff"],
        [((2 * D // count, D), F32), ((D // count, D), F32)],
    )(joined_all, branch, *cot, *up_packs)
    late_moved = over_streams(late_packs)
    head_parts, late_moved[1] = lax.optimization_barrier((head_parts, late_moved[1]))
    (early_part,) = kernel_call(add_kernel, [((4 * HEAD + 8 * share, LANES), BF16)], quarters * "v", megas=24)(
        *head_parts
    )
    early_near = near_blocks(early_part)
    late_moved, early_part = lax.optimization_barrier((late_moved, early_part))
    (late_part,) = kernel_call(add_kernel, [((late_rows, LANES), BF16)], quarters * "v", megas=24)(*late_moved)
    late_near = near_blocks(late_part)
    early_all = far_blocks(early_near)
    late_parts = far_blocks(late_near)
    (grad_frames,) = kernel_call(frames_kernel, [((own, D), F32)], "vvv", megas=24)(
        own_frames, own_cotangent, from_all
    )
    grad_qkv, grad_pos, grad_down, half_up = kernel_call(
        early_kernel,
        [
            ((quarter, 3 * D), F32),
            ((quarter, D), F32),
            ((HALF // quarters, D), F32),
            ((quarter, 2 * HALF), F32, 1, (quarter, HALF), lambda ref: ref.at[:, pl.ds(0, HALF)]),
        ],
        count * "v",
        [((count, 4 * HEAD + 8 * share, LANES), BF16)],
        megas=24,
    )(*early_all)
    late_parts, grad_frames = lax.optimization_barrier((late_parts, grad_frames))
    late = kernel_call(
        late_kernel,
        [((quarter,), F32)] * 6
        + [
            ((quarter, D), F32),
            ((quarter, 2 * HALF), F32, 1, (quarter, HALF), lambda ref: ref.at[:, pl.ds(HALF, HALF)]),
            ((2 * HALF // quarters,), F32),
            ((HALF // quarters,), F32),
            ((HALF // quarters,), F32),
            ((KERNEL, HALF // quarters), F32),
            ((HALF // quarters,), F32),
            ((quarter,), F32),
            ((2 * D // quarters, D), F32),
            ((quarter,), F32),
        ],
        "k" + count * "v",
        [((count,) + late_part.shape, BF16)],
        megas=24,
        aliases={0: 7},
    )(half_up, *late_parts)
    return (
        out_rows[None],
        grad_frames[None],
        *late[:4],
        grad_qkv,
        *late[4:6],
        grad_pos,
        *late[6:13],
        grad_down,
        *late[13:],
    )


def per_device(*operands):
    fits = (
        lax.axis_size("tm") == HEADS
        and lax.axis_size("stream") * LANES == D
        and operands[0].shape[1] == BLOCK
    )
    return head_device(*operands) if fits else frame_device(*operands)


def solution(mesh):
    return jax.shard_map(
        per_device,
        mesh=mesh,
        in_specs=(
            P("stream", "tm", None),
            P("stream", None),
            P("stream", "tm", None),
            P(),
            P(),
            P(),
            P(),
            P(),
            P(),
            P(),
            P(),
            P(),
            P(),
            P(),
            P(),
            P(),
            P(),
            P(),
            P(),
            P(),
            P(),
            P(),
        ),
        out_specs=(
            P("stream", "tm", None),
            P("stream", "tm", None),
            P("stream"),
            P("stream"),
            P("stream"),
            P("stream"),
            P("stream", None),
            P("stream"),
            P("stream"),
            P("stream", None),
            P("stream", None),
            P("stream", None),
            P("stream"),
            P("stream"),
            P("stream"),
            P(None, "stream"),
            P("stream"),
            P("stream", None),
            P("stream"),
            P("stream", None),
            P("stream"),
        ),
        check_vma=False,
    )
```

```python
import math

import jax
import jax.numpy as jnp
from jax import lax
from jax.experimental import pallas as pl
from jax.experimental.pallas import tpu as pltpu
from jax.sharding import PartitionSpec as P

D = 512
HEADS = 8
HEAD = 64
KERNEL = 31
ITEMS = 5
HALF = 1536


EPS = 1e-05
MASKED = -1e30


def extended(block, sides, width):
    for axis, dim in sides:
        count = lax.axis_size(axis)
        forward = [(i, i + 1) for i in range(count - 1)]
        backward = [(target, source) for source, target in forward]
        low = lax.ppermute(
            lax.slice_in_dim(block, block.shape[dim] - width, None, axis=dim), axis, forward
        )
        high = lax.ppermute(lax.slice_in_dim(block, 0, width, axis=dim), axis, backward)
        block = jnp.concatenate([low, block, high], axis=dim)
    return block


def norm_rows(inputs, scale_row, shift_row):
    row_mean = jnp.mean(inputs, axis=-1, keepdims=True)
    centred = inputs - row_mean
    spread = jnp.mean(centred * centred, axis=-1, keepdims=True)
    return centred * lax.rsqrt(spread + EPS) * scale_row + shift_row


def gelu_exact(inputs):
    return jax.nn.gelu(inputs, approximate=False)


def frame_info(lengths, offset, extent):
    item_ends = jnp.cumsum(lengths)
    first_table = jnp.concatenate([item_ends - lengths, item_ends[-1:]])
    frame_index = offset + jnp.arange(extent, dtype=jnp.int32)
    item_of = jnp.sum((frame_index[:, None] >= item_ends[None, :]).astype(jnp.int32), axis=1)
    labels = jnp.arange(ITEMS + 1, dtype=jnp.int32)
    first_frame = jnp.sum(
        jnp.where(item_of[:, None] == labels[None, :], first_table[None, :], 0), axis=1
    )
    return (frame_index, item_of, frame_index - first_frame)


def angles(place_in):
    frequency = jnp.exp(jnp.arange(D // 2, dtype=jnp.float32) * (-2.0 * math.log(10000.0) / D))
    phase_angle = place_in.astype(jnp.float32)[:, None] * frequency[None, :]
    return (jnp.sin(phase_angle), jnp.cos(phase_angle))


def rel_query(projected, sine_rows, cosine_rows):
    half_size = projected.shape[-1] // 2
    first_half = projected[..., :half_size]
    second_half = projected[..., half_size:]
    sine_wide = sine_rows[:, None, :]
    cosine_wide = cosine_rows[:, None, :]
    return jnp.concatenate(
        [
            first_half * sine_wide + second_half * cosine_wide,
            second_half * sine_wide - first_half * cosine_wide,
        ],
        axis=-1,
    )


def step_size(extent):
    return math.gcd(extent, 512)


def score_block(q_content, q_rel, query_item, query_frame, key_block, key_start, lengths):
    extent = key_block.shape[0]
    key_frame, key_item, key_place = frame_info(lengths, key_start, extent)
    sine_rows, cosine_rows = angles(key_place)
    k_rel = jnp.concatenate([cosine_rows, sine_rows], axis=1).astype(jnp.bfloat16)
    raw_scores = jnp.einsum(
        "qhe,khe->hqk",
        q_content,
        key_block.reshape(extent, HEADS, HEAD),
        preferred_element_type=jnp.float32,
    )
    raw_scores = raw_scores + jnp.einsum(
        "qhc,kc->hqk", q_rel, k_rel, preferred_element_type=jnp.float32
    )
    allowed = (query_item[:, None] == key_item[None, :]) & (
        (query_item[:, None] < ITEMS) | (query_frame[:, None] == key_frame[None, :])
    )
    return (raw_scores, allowed, k_rel)


def block_grads(
    q_content,
    q_rel,
    query_item,
    query_frame,
    grad_out,
    log_total,
    delta_rows,
    key_block,
    value_block,
    key_start,
    lengths,
):
    extent = key_block.shape[0]
    raw_scores, allowed, k_rel = score_block(
        q_content, q_rel, query_item, query_frame, key_block, key_start, lengths
    )
    prob_rows = jnp.where(allowed[None], jnp.exp(raw_scores * 0.125 - log_total[:, :, None]), 0.0)
    grad_prob = jnp.einsum(
        "qhe,khe->hqk",
        grad_out,
        value_block.reshape(extent, HEADS, HEAD),
        preferred_element_type=jnp.float32,
    )
    grad_raw = (prob_rows * (grad_prob - delta_rows[:, :, None]) * 0.125).astype(jnp.bfloat16)
    return (prob_rows.astype(jnp.bfloat16), grad_raw, k_rel)


def frame_device(
    frames,
    lengths,
    cotangent,
    ln_attn_gain,
    ln_attn_bias,
    ln_mlp_gain,
    ln_mlp_bias,
    qkv_weight,
    content_bias,
    position_bias,
    pos_weight,
    out_weight,
    up_weight,
    up_bias,
    gate_norm_gain,
    gate_norm_bias,
    conv_kernel,
    conv_bias,
    down_weight,
    down_bias,
    merge_weight,
    merge_bias,
):
    row_count = frames.shape[1]
    cycle_size = lax.axis_size("tm")
    offset = lax.axis_index("tm") * row_count
    stream_lengths = lengths[0]
    inputs = frames[0].astype(jnp.float32)
    frame_index, item_of, place_in = frame_info(stream_lengths, offset, row_count)
    sine_rows, cosine_rows = angles(place_in)
    attn_norm, attn_pull = jax.vjp(
        norm_rows, inputs, ln_attn_gain.astype(jnp.float32), ln_attn_bias.astype(jnp.float32)
    )
    mlp_norm, mlp_pull = jax.vjp(
        norm_rows, inputs, ln_mlp_gain.astype(jnp.float32), ln_mlp_bias.astype(jnp.float32)
    )
    attn_norm_low = attn_norm.astype(jnp.bfloat16)
    mlp_norm_low = mlp_norm.astype(jnp.bfloat16)
    qkv_rows = jnp.dot(attn_norm_low, qkv_weight, preferred_element_type=jnp.float32)
    query_rows = qkv_rows[:, :D]
    key_rows = qkv_rows[:, D : 2 * D].astype(jnp.bfloat16)
    value_rows = qkv_rows[:, 2 * D :].astype(jnp.bfloat16)
    q_content = (query_rows + content_bias.astype(jnp.float32)).astype(jnp.bfloat16)
    q_position = (query_rows + position_bias.astype(jnp.float32)).astype(jnp.bfloat16)
    content_heads = q_content.reshape(row_count, HEADS, HEAD)
    position_heads = q_position.reshape(row_count, HEADS, HEAD)
    pos_heads = pos_weight.reshape(D, HEADS, HEAD)
    projected = jnp.einsum(
        "the,che->thc", position_heads, pos_heads, preferred_element_type=jnp.float32
    )
    q_rel = rel_query(projected, sine_rows, cosine_rows).astype(jnp.bfloat16)
    start_state = (
        jnp.full((HEADS, row_count), MASKED, jnp.float32),
        jnp.zeros((HEADS, row_count), jnp.float32),
        jnp.zeros((HEADS, row_count, HEAD), jnp.float32),
    )
    fold_state = start_state
    key_piece = lax.all_gather(key_rows, "tm", axis=0, tiled=True)
    value_piece = lax.all_gather(value_rows, "tm", axis=0, tiled=True)
    extent = key_piece.shape[0]
    step_rows = step_size(extent)

    def forward_one_step(inner_state, step_index):
        row_top, row_total, row_acc = inner_state
        key_block = lax.dynamic_slice_in_dim(key_piece, step_index * step_rows, step_rows, 0)
        value_block = lax.dynamic_slice_in_dim(value_piece, step_index * step_rows, step_rows, 0)
        raw_scores, allowed, k_rel = score_block(
            content_heads,
            q_rel,
            item_of,
            frame_index,
            key_block,
            step_index * step_rows,
            stream_lengths,
        )
        scaled = jnp.where(allowed[None], raw_scores * 0.125, MASKED)
        new_top = jnp.maximum(row_top, jnp.max(scaled, axis=2))
        weight = jnp.where(allowed[None], jnp.exp(scaled - new_top[:, :, None]), 0.0)
        factor = jnp.exp(row_top - new_top)
        row_total = row_total * factor + jnp.sum(weight, axis=2)
        row_acc = row_acc * factor[:, :, None] + jnp.einsum(
            "hqk,khe->hqe",
            weight.astype(jnp.bfloat16),
            value_block.reshape(step_rows, HEADS, HEAD),
            preferred_element_type=jnp.float32,
        )
        return ((new_top, row_total, row_acc), None)

    fold_state, unused = lax.scan(
        forward_one_step, fold_state, jnp.arange(extent // step_rows, dtype=jnp.int32)
    )
    row_top, row_total, row_acc = fold_state
    attn_heads = row_acc / row_total[:, :, None]
    log_total = row_top + jnp.log(row_total)
    attn_low = jnp.transpose(attn_heads, (1, 0, 2)).reshape(row_count, D).astype(jnp.bfloat16)
    branch_attn = jnp.dot(attn_low, out_weight, preferred_element_type=jnp.float32).astype(
        jnp.bfloat16
    )
    hidden_pre = jnp.dot(
        mlp_norm_low, up_weight, preferred_element_type=jnp.float32
    ) + up_bias.astype(jnp.float32)
    hidden, gelu_pull = jax.vjp(gelu_exact, hidden_pre)
    gate_half = hidden[:, :HALF]
    conv_norm, conv_pull = jax.vjp(
        norm_rows,
        hidden[:, HALF:],
        gate_norm_gain.astype(jnp.float32),
        gate_norm_bias.astype(jnp.float32),
    )
    conv_in = conv_norm.astype(jnp.bfloat16)
    half_width = KERNEL // 2
    conv_wide = extended(conv_in, (("tm", 0),), half_width)
    wide_frame, wide_item, wide_place = frame_info(
        stream_lengths, offset - half_width, row_count + 2 * half_width
    )
    kernel_rows = conv_kernel.astype(jnp.float32)
    conv_out = conv_bias.astype(jnp.float32) + jnp.zeros_like(gate_half)
    for tap_index in range(KERNEL):
        same_item = (wide_item[tap_index : tap_index + row_count] == item_of)[:, None]
        conv_out = (
            conv_out
            + jnp.where(
                same_item, conv_wide[tap_index : tap_index + row_count].astype(jnp.float32), 0.0
            )
            * kernel_rows[tap_index]
        )
    gated_low = (gate_half * conv_out).astype(jnp.bfloat16)
    branch_mlp = (
        jnp.dot(gated_low, down_weight, preferred_element_type=jnp.float32)
        + down_bias.astype(jnp.float32)
    ).astype(jnp.bfloat16)
    joined = jnp.concatenate([branch_attn, branch_mlp], axis=1)
    result = (
        inputs
        + jnp.dot(joined, merge_weight, preferred_element_type=jnp.float32)
        + merge_bias.astype(jnp.float32)
    )
    out_rows = result.astype(jnp.bfloat16)[None]
    grad_low = cotangent[0]
    grad_rows = grad_low.astype(jnp.float32)
    grad_merge_bias = jnp.sum(grad_rows, axis=0)
    grad_merge_weight = jnp.einsum(
        "tc,td->cd", joined, grad_low, preferred_element_type=jnp.float32
    )
    grad_joined = jnp.einsum(
        "td,cd->tc", grad_low, merge_weight, preferred_element_type=jnp.float32
    )
    grad_attn_branch = grad_joined[:, :D].astype(jnp.bfloat16)
    grad_mlp_branch = grad_joined[:, D:].astype(jnp.bfloat16)
    grad_down_weight = jnp.einsum(
        "tc,td->cd", gated_low, grad_mlp_branch, preferred_element_type=jnp.float32
    )
    grad_down_bias = jnp.sum(grad_mlp_branch.astype(jnp.float32), axis=0)
    grad_gated = jnp.einsum(
        "td,cd->tc", grad_mlp_branch, down_weight, preferred_element_type=jnp.float32
    )
    grad_gate_half = grad_gated * conv_out
    grad_conv_out = (grad_gated * gate_half).astype(jnp.bfloat16)
    grad_conv_rows = grad_conv_out.astype(jnp.float32)
    grad_conv_bias = jnp.sum(grad_conv_rows, axis=0)
    grad_wide = extended(grad_conv_out, (("tm", 0),), half_width)
    kernel_list = []
    grad_conv_in = jnp.zeros_like(grad_conv_rows)
    for tap_index in range(KERNEL):
        same_item = (wide_item[tap_index : tap_index + row_count] == item_of)[:, None]
        kernel_list.append(
            jnp.sum(
                jnp.where(
                    same_item, conv_wide[tap_index : tap_index + row_count].astype(jnp.float32), 0.0
                )
                * grad_conv_rows,
                axis=0,
            )
        )
        back_start = 2 * half_width - tap_index
        back_item = (wide_item[back_start : back_start + row_count] == item_of)[:, None]
        grad_conv_in = (
            grad_conv_in
            + jnp.where(
                back_item, grad_wide[back_start : back_start + row_count].astype(jnp.float32), 0.0
            )
            * kernel_rows[tap_index]
        )
    grad_conv_kernel = jnp.stack(kernel_list)
    grad_second, grad_gate_norm_gain, grad_gate_norm_bias = conv_pull(grad_conv_in)
    (grad_pre_rows,) = gelu_pull(jnp.concatenate([grad_gate_half, grad_second], axis=1))
    grad_pre = grad_pre_rows.astype(jnp.bfloat16)
    grad_up_bias = jnp.sum(grad_pre.astype(jnp.float32), axis=0)
    grad_up_weight = jnp.einsum(
        "tc,tf->cf", mlp_norm_low, grad_pre, preferred_element_type=jnp.float32
    )
    grad_mlp_norm = jnp.einsum("tf,cf->tc", grad_pre, up_weight, preferred_element_type=jnp.float32)
    grad_out_weight = jnp.einsum(
        "tc,td->cd", attn_low, grad_attn_branch, preferred_element_type=jnp.float32
    )
    grad_attn_low = jnp.einsum(
        "td,cd->tc", grad_attn_branch, out_weight, preferred_element_type=jnp.float32
    ).astype(jnp.bfloat16)
    grad_out_heads = grad_attn_low.reshape(row_count, HEADS, HEAD)
    delta_rows = jnp.sum(
        jnp.transpose(grad_out_heads.astype(jnp.float32), (1, 0, 2)) * attn_heads, axis=2
    )
    total_frames = row_count * cycle_size
    back_start_state = (
        jnp.zeros((row_count, HEADS, HEAD), jnp.float32),
        jnp.zeros((row_count, HEADS, D), jnp.float32),
        jnp.zeros((total_frames, D), jnp.float32),
        jnp.zeros((total_frames, D), jnp.float32),
    )
    back_key_piece = lax.all_gather(key_rows, "tm", axis=0, tiled=True)
    back_value_piece = lax.all_gather(value_rows, "tm", axis=0, tiled=True)
    extent = back_key_piece.shape[0]
    back_step_rows = step_size(extent)

    def back_one_step(inner_state, step_index):
        grad_content, grad_rel = inner_state
        key_block = lax.dynamic_slice_in_dim(
            back_key_piece, step_index * back_step_rows, back_step_rows, 0
        )
        value_block = lax.dynamic_slice_in_dim(
            back_value_piece, step_index * back_step_rows, back_step_rows, 0
        )
        prob_low, grad_raw, k_rel = block_grads(
            content_heads,
            q_rel,
            item_of,
            frame_index,
            grad_out_heads,
            log_total,
            delta_rows,
            key_block,
            value_block,
            step_index * back_step_rows,
            stream_lengths,
        )
        grad_content = grad_content + jnp.einsum(
            "hqk,khe->qhe",
            grad_raw,
            key_block.reshape(back_step_rows, HEADS, HEAD),
            preferred_element_type=jnp.float32,
        )
        grad_rel = grad_rel + jnp.einsum(
            "hqk,kc->qhc", grad_raw, k_rel, preferred_element_type=jnp.float32
        )
        key_part = jnp.einsum(
            "hqk,qhe->khe", grad_raw, content_heads, preferred_element_type=jnp.float32
        ).reshape(back_step_rows, D)
        value_part = jnp.einsum(
            "hqk,qhe->khe", prob_low, grad_out_heads, preferred_element_type=jnp.float32
        ).reshape(back_step_rows, D)
        return ((grad_content, grad_rel), (key_part, value_part))

    inner_state, block_parts = lax.scan(
        back_one_step,
        (back_start_state[0], back_start_state[1]),
        jnp.arange(extent // back_step_rows, dtype=jnp.int32),
    )
    key_all = block_parts[0].reshape(extent, D)
    value_all = block_parts[1].reshape(extent, D)
    grad_content, grad_rel, key_all, value_all = (
        inner_state[0],
        inner_state[1],
        key_all,
        value_all,
    )
    grad_keys, grad_values = (
        lax.psum_scatter(key_all, "tm", scatter_dimension=0, tiled=True),
        lax.psum_scatter(value_all, "tm", scatter_dimension=0, tiled=True),
    )
    half_size = D // 2
    rel_first = grad_rel[..., :half_size]
    rel_second = grad_rel[..., half_size:]
    sine_wide = sine_rows[:, None, :]
    cosine_wide = cosine_rows[:, None, :]
    grad_projected = jnp.concatenate(
        [
            rel_first * sine_wide - rel_second * cosine_wide,
            rel_first * cosine_wide + rel_second * sine_wide,
        ],
        axis=-1,
    ).astype(jnp.bfloat16)
    grad_pos_weight = jnp.einsum(
        "thc,the->che", grad_projected, position_heads, preferred_element_type=jnp.float32
    ).reshape(D, D)
    grad_q_position = jnp.einsum(
        "thc,che->the", grad_projected, pos_heads, preferred_element_type=jnp.float32
    )
    grad_content_bias = jnp.sum(grad_content, axis=0).reshape(D)
    grad_position_bias = jnp.sum(grad_q_position, axis=0).reshape(D)
    grad_query = (grad_content + grad_q_position).reshape(row_count, D).astype(jnp.bfloat16)
    grad_qkv = jnp.concatenate(
        [grad_query, grad_keys.astype(jnp.bfloat16), grad_values.astype(jnp.bfloat16)], axis=1
    )
    grad_qkv_weight = jnp.einsum(
        "tc,tf->cf", attn_norm_low, grad_qkv, preferred_element_type=jnp.float32
    )
    grad_attn_norm = jnp.einsum(
        "tf,cf->tc", grad_qkv, qkv_weight, preferred_element_type=jnp.float32
    )
    grad_from_attn, grad_ln_attn_gain, grad_ln_attn_bias = attn_pull(grad_attn_norm)
    grad_from_mlp, grad_ln_mlp_gain, grad_ln_mlp_bias = mlp_pull(grad_mlp_norm)
    grad_inputs = grad_rows + grad_from_attn + grad_from_mlp
    weight_grads = (
        grad_ln_attn_gain,
        grad_ln_attn_bias,
        grad_ln_mlp_gain,
        grad_ln_mlp_bias,
        grad_qkv_weight,
        grad_content_bias,
        grad_position_bias,
        grad_pos_weight,
        grad_out_weight,
        grad_up_weight,
        grad_up_bias,
        grad_gate_norm_gain,
        grad_gate_norm_bias,
        grad_conv_kernel,
        grad_conv_bias,
        grad_down_weight,
        grad_down_bias,
        grad_merge_weight,
        grad_merge_bias,
    )
    summed = lax.psum(
        (
            weight_grads[0],
            weight_grads[1],
            weight_grads[2],
            weight_grads[3],
            weight_grads[4],
            weight_grads[5],
            weight_grads[6],
            weight_grads[7],
            weight_grads[8],
            weight_grads[9],
            weight_grads[10],
            weight_grads[11],
            weight_grads[12],
            weight_grads[13],
            weight_grads[14],
            weight_grads[15],
            weight_grads[16],
            weight_grads[17],
            weight_grads[18],
        ),
        "tm",
    )
    shares = (
        lax.psum_scatter(
            summed[0].astype(jnp.bfloat16), "stream", scatter_dimension=0, tiled=True
        ).astype(jnp.float32),
        lax.psum_scatter(
            summed[1].astype(jnp.bfloat16), "stream", scatter_dimension=0, tiled=True
        ).astype(jnp.float32),
        lax.psum_scatter(
            summed[2].astype(jnp.bfloat16), "stream", scatter_dimension=0, tiled=True
        ).astype(jnp.float32),
        lax.psum_scatter(
            summed[3].astype(jnp.bfloat16), "stream", scatter_dimension=0, tiled=True
        ).astype(jnp.float32),
        lax.psum_scatter(
            summed[4].astype(jnp.bfloat16), "stream", scatter_dimension=0, tiled=True
        ).astype(jnp.float32),
        lax.psum_scatter(
            summed[5].astype(jnp.bfloat16), "stream", scatter_dimension=0, tiled=True
        ).astype(jnp.float32),
        lax.psum_scatter(
            summed[6].astype(jnp.bfloat16), "stream", scatter_dimension=0, tiled=True
        ).astype(jnp.float32),
        lax.psum_scatter(
            summed[7].astype(jnp.bfloat16), "stream", scatter_dimension=0, tiled=True
        ).astype(jnp.float32),
        lax.psum_scatter(
            summed[8].astype(jnp.bfloat16), "stream", scatter_dimension=0, tiled=True
        ).astype(jnp.float32),
        lax.psum_scatter(
            summed[9].astype(jnp.bfloat16), "stream", scatter_dimension=0, tiled=True
        ).astype(jnp.float32),
        lax.psum_scatter(
            summed[10].astype(jnp.bfloat16), "stream", scatter_dimension=0, tiled=True
        ).astype(jnp.float32),
        lax.psum_scatter(
            summed[11].astype(jnp.bfloat16), "stream", scatter_dimension=0, tiled=True
        ).astype(jnp.float32),
        lax.psum_scatter(
            summed[12].astype(jnp.bfloat16), "stream", scatter_dimension=0, tiled=True
        ).astype(jnp.float32),
        lax.psum_scatter(
            summed[13].astype(jnp.bfloat16), "stream", scatter_dimension=1, tiled=True
        ).astype(jnp.float32),
        lax.psum_scatter(
            summed[14].astype(jnp.bfloat16), "stream", scatter_dimension=0, tiled=True
        ).astype(jnp.float32),
        lax.psum_scatter(
            summed[15].astype(jnp.bfloat16), "stream", scatter_dimension=0, tiled=True
        ).astype(jnp.float32),
        lax.psum_scatter(
            summed[16].astype(jnp.bfloat16), "stream", scatter_dimension=0, tiled=True
        ).astype(jnp.float32),
        lax.psum_scatter(
            summed[17].astype(jnp.bfloat16), "stream", scatter_dimension=0, tiled=True
        ).astype(jnp.float32),
        lax.psum_scatter(
            summed[18].astype(jnp.bfloat16), "stream", scatter_dimension=0, tiled=True
        ).astype(jnp.float32),
    )
    return (out_rows, grad_inputs[None]) + tuple(shares)


LANES = 128
LOW = LANES // 2
BLOCK = 128
TALL = 256
WINDOW = 64
MARGIN = 16
BOUNDS = 16
MEGA = 1024 * 1024
F32 = jnp.float32
BF16 = jnp.bfloat16


def dot_nn(left, right):
    return jnp.dot(left, right, preferred_element_type=F32)


def dot_nt(left, right):
    return lax.dot_general(left, right, (((1,), (1,)), ((), ())), preferred_element_type=F32)


def dot_tn(left, right):
    return lax.dot_general(left, right, (((0,), (0,)), ((), ())), preferred_element_type=F32)


def rows_of(index, size, base=0):
    return pl.ds(pl.multiple_of(index * size, size) + base, size)


def line_of(ref):
    return ref[...].astype(F32).reshape(1, ref.shape[0])


def fold_rows(values):
    return jnp.sum(values.reshape(values.shape[0] // 8, 8, values.shape[1]), axis=0)


def one_row(values):
    return jnp.sum(values, axis=0, keepdims=True)


def turn(values):
    return pltpu.roll(values, LOW, 1)


def low_lanes(rows):
    return lax.broadcasted_iota(jnp.int32, (rows, LANES), 1) < LOW


def centre_rows(inputs):
    mean = jnp.mean(inputs, axis=-1, keepdims=True)
    centred = inputs - mean
    spread = jnp.mean(centred * centred, axis=-1, keepdims=True)
    return centred * lax.rsqrt(spread + EPS)


def gelu_parts(values):
    phi = 0.5 + 0.5 * lax.erf(values * math.sqrt(0.5))
    bell = jnp.exp(values * values * -0.5)
    return values * phi, phi + values * bell * (1.0 / math.sqrt(2.0 * math.pi))


class Part:
    def __init__(self, shape=None, pairs=None, refs=1, late=False):
        self.shape, self.pairs, self.refs, self.late = shape, pairs, refs, late

    def buffer(self, operand):
        return self.shape or operand.shape

    def copies(self, refs, buffer):
        return self.pairs(refs, buffer) if self.pairs else [(refs[0], buffer)]


def blocks_part(late=False):
    def pairs(refs, buffer):
        place = lax.axis_index("tm")
        return [
            (ref, buffer.at[rows_of(lax.bitwise_xor(jnp.int32(apart), place), BLOCK)])
            for apart, ref in enumerate(refs)
        ]

    return Part((HEADS * BLOCK, D), pairs, HEADS, late)


def rows_part(first, size, late=False):
    return Part((size, D), lambda refs, buffer: [(refs[0].at[pl.ds(first, size)], buffer)], late=late)


class Fetch:
    def __init__(self, pairs, buffer, sems, first):
        self.buffer, self.begun = buffer, False
        self.pending = [
            pltpu.make_async_copy(source, target, sems.at[first + index])
            for index, (source, target) in enumerate(pairs)
        ]

    def begin(self):
        if not self.begun:
            for copy in self.pending:
                copy.start()
        self.begun = True

    def __call__(self):
        self.begin()
        for copy in self.pending:
            copy.wait()
        self.pending = []
        return self.buffer


def begin(*fetches):
    for fetch in fetches:
        fetch.begin()


class Send:
    def __init__(self, buffer, target, sems):
        self.buffer, self.target, self.sems, self.copies = buffer, target, sems, []

    def go(self, *index):
        source, target = (self.buffer.at[index], self.target.at[index]) if index else (self.buffer, self.target)
        copy = pltpu.make_async_copy(source, target, self.sems[len(self.copies)])
        copy.start()
        self.copies.append(copy)

    def finish(self):
        if not self.copies:
            self.go()


SPACES = {"v": pltpu.VMEM, "s": pltpu.SMEM, "k": pl.ANY}


def kernel_call(body, out_shapes, plan, scratch=(), megas=58, bounds=False, aliases=None):
    def call(*operands):
        in_specs, buffers, at = [], [], 0
        for item in plan:
            if item == "f":
                in_specs.append(pl.BlockSpec(memory_space=pl.ANY))
                buffers.append(pltpu.VMEM(operands[at].shape, operands[at].dtype))
                at += 1
            elif isinstance(item, Part):
                in_specs += [pl.BlockSpec(memory_space=pl.ANY)] * item.refs
                buffers.append(pltpu.VMEM(item.buffer(operands[at]), operands[at].dtype))
                at += item.refs
            else:
                in_specs.append(pl.BlockSpec(memory_space=SPACES[item]))
                at += 1
        sent = [out for out in out_shapes if len(out) > 2]
        buffers += [pltpu.VMEM(out[3] if len(out) > 3 else out[0], out[1]) for out in sent]
        sem_count = 96
        extra = [pltpu.SMEM((BOUNDS,), jnp.int32)] if bounds else []

        def outer(*refs):
            inputs, rest = refs[: len(in_specs)], refs[len(in_specs) :]
            outputs, rest = rest[: len(out_shapes)], rest[len(out_shapes) :]
            held, rest = list(rest[: len(buffers)]), rest[len(buffers) :]
            sems, rest = rest[0], rest[1:]
            given, at, used = [], 0, 0
            for item in plan:
                if item == "f":
                    given.append(Fetch([(inputs[at], held[0])], held.pop(0), sems, used))
                    given[-1].begin()
                    used += 1
                    at += 1
                elif isinstance(item, Part):
                    buffer = held.pop(0)
                    pairs = item.copies(inputs[at : at + item.refs], buffer)
                    given.append(Fetch(pairs, buffer, sems, used))
                    if not item.late:
                        given[-1].begin()
                    used += len(pairs)
                    at += item.refs
                else:
                    given.append(inputs[at])
                    at += 1
            results = []
            for out, ref in zip(out_shapes, outputs):
                if len(out) > 2:
                    target = out[4](ref) if len(out) > 3 else ref
                    results.append(Send(held.pop(0), target, [sems.at[used + index] for index in range(4)]))
                    used += 4
                else:
                    results.append(ref)
            assert used <= sem_count
            given = [item() if kind == "f" else item for kind, item in zip(plan, given)]
            body(*given, *results, *rest)
            for item in given:
                if isinstance(item, Fetch):
                    item()
            sends = [item for item in results if isinstance(item, Send)]
            for item in sends:
                item.finish()
            for item in sends:
                for copy in item.copies:
                    copy.wait()

        return pl.pallas_call(
            outer,
            out_shape=[jax.ShapeDtypeStruct(out[0], out[1]) for out in out_shapes],
            in_specs=in_specs,
            out_specs=[pl.BlockSpec(memory_space=pl.ANY if len(out) > 2 else pltpu.VMEM) for out in out_shapes],
            scratch_shapes=buffers
            + [pltpu.SemaphoreType.DMA((sem_count,))]
            + [pltpu.VMEM(shape, kind) for shape, kind in scratch]
            + extra,
            input_output_aliases=aliases or {},
            compiler_params=pltpu.CompilerParams(vmem_limit_bytes=megas * MEGA),
            cost_estimate=pl.CostEstimate(flops=0, bytes_accessed=0, transcendentals=0),
        )(*operands)

    return call


def fill_bounds(lengths_ref, bounds_s, total):
    bounds_s[0] = jnp.int32(0)
    end = jnp.int32(0)
    for item in range(ITEMS):
        end = end + lengths_ref[0, item]
        bounds_s[item + 1] = end
    for item in range(ITEMS + 1, BOUNDS):
        bounds_s[item] = jnp.int32(total)


def select_kernel(
    up_ref,
    up_bias_ref,
    gain_ref,
    bias_ref,
    conv_bias_ref,
    taps_ref,
    qkv_ref,
    pos_ref,
    content_ref,
    position_ref,
    up_out,
    table_out,
    qkv_out,
    pos_out,
    bias_out,
):
    place = lax.axis_index("tm")
    quarters = lax.axis_size("stream")
    share = HALF // (quarters * lax.axis_size("tm"))
    lane = lax.broadcasted_iota(jnp.int32, (1, 2 * LANES), 1)
    channel = jnp.where(lane < LANES + LOW, lane, lane - LOW)
    group = jnp.zeros_like(channel)
    for quarter in range(1, quarters):
        group = group + (channel >= quarter * share).astype(jnp.int32)
    source = group * (HALF // quarters) + share * place + channel - group * share
    chosen = (lax.broadcasted_iota(jnp.int32, (HALF, 2 * LANES), 0) == source).astype(F32).astype(BF16)
    gate = dot_nn(up_ref[:, :HALF], chosen)
    conv = dot_nn(up_ref[:, HALF:], chosen)
    up_out[:, :LANES] = gate[:, :LANES].astype(BF16)
    up_out[:, LANES : 2 * LANES] = jnp.where(low_lanes(D), gate[:, LANES:], conv[:, LANES:]).astype(BF16)
    up_out[:, 2 * LANES :] = conv[:, :LANES].astype(BF16)
    up_bias = line_of(up_bias_ref)
    lines = jnp.concatenate(
        [
            up_bias[:, :HALF],
            up_bias[:, HALF:],
            line_of(gain_ref),
            line_of(bias_ref),
            line_of(conv_bias_ref),
            jnp.zeros((3, HALF), F32),
        ],
        axis=0,
    )
    lines = dot_nn(lines.astype(BF16), chosen)
    taps = dot_nn(taps_ref[...], chosen)
    for part in range(2):
        lanes = slice(part * LANES, (part + 1) * LANES)
        table_out[part, :8] = lines[:, lanes]
        table_out[part, 8 : 8 + KERNEL] = taps[:, lanes]
        table_out[part, 8 + KERNEL :] = jnp.zeros((1, LANES), F32)

    odd = lax.rem(place, 2) == 1

    def head_lanes(ref, base):
        at = pl.ds(pl.multiple_of(lax.div(place, 2) * LANES + base, LANES), LANES)
        values = ref[:, at].astype(F32)
        values = jnp.where(odd, turn(values), values)
        return jnp.where(low_lanes(values.shape[0]), values, 0.0)

    for part in range(3):
        qkv_out[:, part * LANES : (part + 1) * LANES] = head_lanes(qkv_ref, part * D).astype(BF16)
    pos_out[...] = head_lanes(pos_ref, 0).astype(BF16)
    bias_out[...] = jnp.zeros((8, LANES), F32)
    for line, ref in enumerate((content_ref, position_ref)):
        values = line_of(ref)
        picked = values[:, :LANES]
        for tile in range(1, D // LANES):
            picked = jnp.where(
                lax.div(place, 2) == tile, values[:, tile * LANES : (tile + 1) * LANES], picked
            )
        picked = jnp.where(odd, turn(picked), picked)
        bias_out[line : line + 1] = jnp.where(low_lanes(1), picked, 0.0)


def angle_rows(coarse_ref, fine_ref, block, rows):
    half = D // 2
    base = coarse_ref[pl.ds(block, 1)]
    base_sine, base_cosine = base[:, :half], base[:, half:]
    sine, cosine = fine_ref[rows, :half], fine_ref[rows, half:]
    return base_sine * cosine + base_cosine * sine, base_cosine * cosine - base_sine * sine


def item_codes(bounds_s, index):
    code = jnp.zeros_like(index)
    for item in range(1, ITEMS + 1):
        code = code + (index >= bounds_s[item]).astype(jnp.int32)
    return jnp.where(code < ITEMS, code, ITEMS + index)


def attend_kernel(
    lengths_ref,
    x_ref,
    attn_gain_ref,
    attn_bias_ref,
    mlp_gain_ref,
    mlp_bias_ref,
    qkv_ref,
    pos_ref,
    bias_ref,
    coarse_ref,
    fine_ref,
    up_ref,
    up_bias_ref,
    n_attn_out,
    n_mlp_out,
    hat_out,
    q_position_out,
    query_out,
    key_out,
    value_out,
    prob_out,
    attn_out,
    stats_out,
    bounds_s,
):
    frames = n_attn_out.buffer.shape[0]
    half = D // 2
    fill_bounds(lengths_ref, bounds_s, frames)
    attn_gain, attn_bias = line_of(attn_gain_ref), line_of(attn_bias_ref)
    mlp_gain, mlp_bias = line_of(mlp_gain_ref), line_of(mlp_bias_ref)
    content, position = bias_ref[0:1], bias_ref[1:2]
    x_ref = x_ref()
    begin(up_ref)

    @pl.loop(0, frames // TALL, unroll=4)
    def _(block):
        rows = rows_of(block, TALL)
        for part in range(TALL // 32):
            at = pl.ds(pl.multiple_of(block * TALL + part * 32, 32), 32)
            hat = centre_rows(x_ref[at].astype(F32))
            hat_out.buffer[at] = hat.astype(BF16)
            n_attn_out.buffer[at] = (hat * attn_gain + attn_bias).astype(BF16)
            n_mlp_out.buffer[at] = (hat * mlp_gain + mlp_bias).astype(BF16)
        parts = dot_nn(n_attn_out.buffer[rows], qkv_ref[...])
        query = parts[:, :LANES]
        query_out.buffer[rows, :LANES] = ((query + content).astype(BF16).astype(F32) * 0.125).astype(BF16)
        q_position = (query + position).astype(BF16)
        q_position_out.buffer[rows] = q_position
        key_out.buffer[rows, :LANES] = parts[:, LANES : 2 * LANES].astype(BF16)
        value_out.buffer[rows] = parts[:, 2 * LANES :].astype(BF16)
        projected = dot_nt(q_position, pos_ref[...])
        for part in range(TALL // 32):
            at = pl.ds(pl.multiple_of(block * TALL + part * 32, 32), 32)
            inner = part * 32 % BLOCK
            sine, cosine = angle_rows(
                coarse_ref, fine_ref, block * (TALL // BLOCK) + part * 32 // BLOCK, slice(inner, inner + 32)
            )
            first = projected[part * 32 : part * 32 + 32, :half]
            second = projected[part * 32 : part * 32 + 32, half:]
            query_out.buffer[at, LANES : LANES + half] = ((first * sine + second * cosine) * 0.125).astype(BF16)
            query_out.buffer[at, LANES + half :] = ((second * sine - first * cosine) * 0.125).astype(BF16)
            key_out.buffer[at, LANES : LANES + half] = cosine.astype(BF16)
            key_out.buffer[at, LANES + half :] = sine.astype(BF16)

    for out in (n_attn_out, n_mlp_out, hat_out, q_position_out, query_out, key_out, value_out):
        out.go()
    up_ref = up_ref()
    up_bias = line_of(up_bias_ref)[:, HALF:]
    lane = lax.broadcasted_iota(jnp.int32, (16, LANES), 1)

    @pl.loop(0, frames // TALL, unroll=2)
    def _(block):
        values = dot_nn(n_mlp_out.buffer[rows_of(block, TALL)], up_ref[...])
        for part in range(TALL // 16):
            pre = values[part * 16 : part * 16 + 16] + up_bias
            hidden = pre * (0.5 + 0.5 * lax.erf(pre * math.sqrt(0.5)))
            mean = jnp.mean(hidden, axis=-1, keepdims=True)
            centred = hidden - mean
            rate = lax.rsqrt(jnp.mean(centred * centred, axis=-1, keepdims=True) + EPS)
            at = pl.ds(pl.multiple_of(block * TALL + part * 16, 16), 16)
            stats_out.buffer[at] = jnp.where(lane == 0, mean, rate)

    stats_out.go()
    key_code = item_codes(bounds_s, lax.broadcasted_iota(jnp.int32, (1, frames), 1))

    low = low_lanes(32)
    for block in range(frames // TALL):
        rows = pl.ds(block * TALL, TALL)
        raw = dot_nt(query_out.buffer[rows], key_out.buffer[...])
        shares = []
        for part in range(TALL // 32):
            start = block * TALL + part * 32
            index = start + lax.broadcasted_iota(jnp.int32, (32, 1), 0)
            scaled = jnp.where(
                item_codes(bounds_s, index) == key_code, raw[part * 32 : part * 32 + 32], MASKED
            )
            weight = jnp.exp(scaled - jnp.max(scaled, axis=1, keepdims=True))
            prob_out.buffer[pl.ds(start, 32)] = weight.astype(BF16)
            shares.append(1.0 / jnp.sum(weight, axis=1, keepdims=True))
        prob_out.go(rows)
        attn = dot_nn(prob_out.buffer[rows], value_out.buffer[...])
        for part in range(TALL // 32):
            share = shares[part]
            attn_out.buffer[pl.ds(block * TALL + part * 32, 32)] = jnp.where(
                low, attn[part * 32 : part * 32 + 32] * share, share
            )


def fill_margins(wide_s, frames):
    edge = jnp.zeros((MARGIN, LANES), F32)
    wide_s[:MARGIN] = edge
    wide_s[MARGIN + frames : 2 * MARGIN + frames] = edge
    base = frames + 3 * MARGIN
    after = base + frames // 2
    low = low_lanes(MARGIN)
    wide_s[base - MARGIN : base] = jnp.where(low, 0.0, turn(wide_s[after - MARGIN : after]))
    wide_s[after : after + MARGIN] = jnp.where(low, turn(wide_s[base : base + MARGIN]), 0.0)


def item_span(bounds_s, frame):
    begin, end = bounds_s[0], bounds_s[BOUNDS - 1]
    for item in range(1, ITEMS + 1):
        edge = bounds_s[item]
        begin = jnp.where(frame >= edge, edge, begin)
    for item in range(ITEMS, 0, -1):
        edge = bounds_s[item]
        end = jnp.where(frame < edge, edge, end)
    return begin, end


def is_whole(bounds_s, start):
    begin, end = item_span(bounds_s, start)
    reach = KERNEL // 2
    low = (begin == 0) | (begin <= start - reach)
    high = (end == bounds_s[BOUNDS - 1]) | (end >= start + WINDOW + reach)
    return low & high & (end >= start + WINDOW)


def tap_limits(bounds_s, start):
    frame = start + lax.broadcasted_iota(jnp.int32, (WINDOW, LANES), 0)
    begin, end = item_span(bounds_s, frame)
    return begin - frame, end - frame


def grouped(values):
    return values.reshape(WINDOW // 8, 8, LANES)


def triple_places(step, frames):
    half = frames // 2
    return (
        pl.multiple_of(step * WINDOW, 2 * MARGIN),
        pl.multiple_of(step * WINDOW + half, 2 * MARGIN),
        pl.multiple_of(step * WINDOW + frames + 2 * MARGIN, 2 * MARGIN),
    )


def over_windows(bounds_s, frames, body):
    half = frames // 2

    @pl.loop(0, half // WINDOW)
    def _(step):
        start = step * WINDOW
        whole = is_whole(bounds_s, start) & is_whole(bounds_s, start + half)

        @pl.when(whole)
        def _():
            body(step, None)

        @pl.when(jnp.logical_not(whole))
        def _():
            first, second = tap_limits(bounds_s, start), tap_limits(bounds_s, start + half)
            low = low_lanes(WINDOW)
            rest = [jnp.where(low, one, other) for one, other in zip(first, second)]
            body(step, (first, second, rest))


def tap_view(window_ref, tap, limits):
    view = window_ref[tap + 1 : tap + 1 + WINDOW]
    if limits is not None:
        shift = tap - KERNEL // 2
        view = jnp.where((limits[0] <= shift) & (limits[1] > shift), view, 0.0)
    return grouped(view)


def mlp_first_kernel(
    lengths_ref,
    n_ref,
    up_ref,
    table_ref,
    stats_ref,
    cot_ref,
    merge_ref,
    down_ref,
    attn_ref,
    mixed_out,
    gate_pre_out,
    grad_out,
    rate_out,
    hat_out,
    early_out,
    vectors_out,
    lines_out,
    hat_s,
    slope_s,
    gate_s,
    hidden_s,
    gate_slope_s,
    conv_s,
    grad_s,
    out_s,
    back_s,
    branch_s,
    mix_s,
    taps_s,
    turn_s,
    tap_sum_s,
    columns_s,
    forward_s,
    backward_s,
    bounds_s,
):
    frames = mix_s.shape[0]
    half = frames // 2
    blocks = frames // BLOCK
    quarters, early_rows, _ = early_out.buffer.shape
    share = early_rows // 8
    channels = quarters * share
    fill_bounds(lengths_ref, bounds_s, frames)
    for part in range(2):
        for tap in range(KERNEL):
            line = jnp.broadcast_to(table_ref[part, 8 + tap : 9 + tap], (8, LANES))
            taps_s[part, tap] = line
            turn_s[part, KERNEL - 1 - tap] = line
    tap_sum_s[...] = jnp.zeros(tap_sum_s.shape, F32)
    main, rest = table_ref[0, :8], table_ref[1, :8]
    mixed_bias = jnp.where(low_lanes(1), rest[0:1], rest[1:2])
    low = low_lanes(64)
    gate_pre_ref = gate_pre_out.buffer
    n_ref = n_ref()
    stats_ref = stats_ref()
    begin(cot_ref, merge_ref, down_ref, attn_ref)

    def stat_rows(rows):
        stats = stats_ref[rows]
        return stats[:, 0:1], stats[:, 1:2]

    def chunk(start, base=0):
        return pl.ds(pl.multiple_of(start, 64) + base, 64)

    def conv_part(hidden, mean, rate, lines, rows, to_rows):
        hat = (hidden - mean) * rate
        hat_s[rows] = hat
        hat_out.buffer[rows] = hat.astype(BF16)
        conv_s[to_rows] = (hat * lines[2:3] + lines[3:4]).astype(BF16).astype(F32)

    @pl.loop(0, half // TALL, unroll=2)
    def _(block):
        pre = [dot_nn(n_ref[rows_of(block, TALL, base)], up_ref[...]) for base in (0, half)]
        for part in range(TALL // 64):
            inner = slice(part * 64, part * 64 + 64)
            start = block * TALL + part * 64
            mixed = []
            for values, base in zip(pre, (0, half)):
                rows = chunk(start, base)
                gate, gate_slope = gelu_parts(values[inner, :LANES] + main[0:1])
                hidden_s[rows] = gate
                gate_slope_s[rows] = gate_slope
                hidden, slope = gelu_parts(values[inner, 2 * LANES :] + main[1:2])
                mean, rate = stat_rows(rows)
                slope_s[rows] = slope * rate
                conv_part(hidden, mean, rate, main, rows, chunk(start, base + MARGIN))
                mixed.append((*gelu_parts(values[inner, LANES : 2 * LANES] + mixed_bias), mean, rate))
            (low_hidden, low_slope, low_mean, low_rate), (high_hidden, high_slope, high_mean, high_rate) = mixed
            rows = chunk(start, frames)
            hidden_s[rows] = jnp.where(low, low_hidden, turn(high_hidden))
            gate_slope_s[rows] = jnp.where(low, low_slope, turn(high_slope))
            rate = jnp.where(low, low_rate, high_rate)
            slope_s[rows] = jnp.where(low, turn(low_slope), high_slope) * rate
            conv_part(
                jnp.where(low, turn(low_hidden), high_hidden),
                jnp.where(low, low_mean, high_mean),
                rate,
                rest,
                rows,
                chunk(start, frames + 3 * MARGIN),
            )

    hat_out.go()
    fill_margins(conv_s, frames)
    tall = WINDOW + 2 * MARGIN
    outs = (0, half, frames)

    def convolve(step, limits):
        for index, base in enumerate(triple_places(step, frames)):
            forward_s[index] = conv_s[pl.ds(base, tall)]
        for index in range(3):
            own = None if limits is None else limits[index]
            total = jnp.zeros((WINDOW // 8, 8, LANES), F32)
            for tap in range(KERNEL):
                total = total + tap_view(forward_s.at[index], tap, own) * taps_s[index // 2, tap][None]
            lines = rest if index == 2 else main
            out_s[rows_of(step, WINDOW, outs[index])] = total.reshape(WINDOW, LANES) + lines[4:5]

    over_windows(bounds_s, frames, convolve)
    cot_ref = cot_ref()
    merge_ref = merge_ref()
    down_ref = down_ref()
    attn_ref = attn_ref()
    down_ref[channels:] = jnp.zeros((2 * LANES - channels, D), BF16)
    zero = jnp.zeros((8, LANES), F32)

    def branch_part(grad_gated, rows, to_rows, sums):
        up_sum, conv_sum = sums
        gate, conv = hidden_s[rows], out_s[rows]
        gate_pre = (grad_gated * conv * gate_slope_s[rows]).astype(BF16)
        gate_pre_ref[rows] = gate_pre
        grad_conv = (grad_gated * gate).astype(BF16).astype(F32)
        grad_s[to_rows] = grad_conv
        gate_pre = gate_pre.astype(F32)
        return gate * conv, gate_pre, (up_sum + fold_rows(gate_pre), conv_sum + fold_rows(grad_conv))

    def branch_step(block, sums):
        main_sums, rest_sums = sums
        grads = []
        for base in (0, half):
            rows = rows_of(block, TALL, base)
            branch = dot_nt(cot_ref[rows], merge_ref[...]).astype(BF16)
            branch_s[rows] = branch
            grads.append(dot_nt(branch, down_ref[...]))
        for part in range(TALL // 64):
            inner = slice(part * 64, part * 64 + 64)
            start = block * TALL + part * 64
            for values, base in zip(grads, (0, half)):
                rows = chunk(start, base)
                gated, gate_pre, main_sums = branch_part(
                    values[inner, :LANES], rows, chunk(start, base + MARGIN), main_sums
                )
                mix_s[rows, :LANES] = gated.astype(BF16)
                gate_s[rows, :LANES] = gate_pre.astype(BF16)
            grad = jnp.where(low, grads[0][inner, LANES:], turn(grads[1][inner, LANES:]))
            gated, gate_pre, rest_sums = branch_part(
                grad, chunk(start, frames), chunk(start, frames + 3 * MARGIN), rest_sums
            )
            low_rows, high_rows = chunk(start), chunk(start, half)
            gate_s[low_rows, LANES:] = gate_pre.astype(BF16)
            gate_s[high_rows, LANES:] = turn(gate_pre).astype(BF16)
            mix_s[low_rows, LANES:] = jnp.where(low, gated, turn(attn_ref[low_rows])).astype(BF16)
            mix_s[high_rows, LANES:] = jnp.where(low, turn(gated), turn(attn_ref[high_rows])).astype(BF16)
        return main_sums, rest_sums

    (main_up, main_conv), (rest_up, rest_conv) = lax.fori_loop(
        0, half // TALL, branch_step, ((zero, zero), (zero, zero)), unroll=2
    )
    gate_pre_out.go()
    fill_margins(grad_s, frames)
    ones = jnp.ones((16, frames), BF16)
    lines_out[0:1] = dot_nn(ones, branch_s[...])[0:1]
    lines_out[1:2] = dot_nn(ones, cot_ref[...])[0:1]
    lines_out[2:8] = jnp.zeros((6, D), F32)
    grad_down = dot_tn(mix_s[...], branch_s[...])
    grad_gate = dot_tn(gate_s[...], n_ref[...])
    for quarter in range(quarters):
        for tile in range(4):
            early_out.buffer[quarter, tile * share : (tile + 1) * share] = grad_down[
                quarter * share : (quarter + 1) * share, tile * LANES : (tile + 1) * LANES
            ].astype(BF16)
        early_out.buffer[quarter, 4 * share :] = grad_gate[
            :channels, quarter * LANES : (quarter + 1) * LANES
        ].astype(BF16)
    early_out.go()
    for block in range(blocks):
        mixed_out.buffer[block, :BLOCK] = mix_s[block * BLOCK : (block + 1) * BLOCK]
    mixed_out.go(slice(None), pl.ds(0, BLOCK))

    def differentiate(step, limits):
        for index, base in enumerate(triple_places(step, frames)):
            forward_s[index] = conv_s[pl.ds(base, tall)]
            backward_s[index] = grad_s[pl.ds(base, tall)]
        for index in range(3):
            own = None if limits is None else limits[index]
            total = jnp.zeros((WINDOW // 8, 8, LANES), F32)
            centre = grouped(backward_s[index, MARGIN : MARGIN + WINDOW])
            for tap in range(KERNEL):
                total = total + tap_view(backward_s.at[index], tap, own) * turn_s[index // 2, tap][None]
                tap_sum_s[index // 2, tap] += jnp.sum(tap_view(forward_s.at[index], tap, own) * centre, axis=0)
            back_s[rows_of(step, WINDOW, outs[index])] = total.reshape(WINDOW, LANES)

    over_windows(bounds_s, frames, differentiate)
    lane = lax.broadcasted_iota(jnp.int32, (64, LANES), 1)

    def norm_part(rows, lines, sums):
        gain_sum, bias_sum = sums
        back, hat, slope = back_s[rows], hat_s[rows], slope_s[rows]
        grad = back * lines[2:3]
        grad_out.buffer[rows] = (grad * slope).astype(BF16)
        rate_out.buffer[rows] = slope.astype(BF16)
        along = back * hat
        return grad, along * lines[2:3], (gain_sum + fold_rows(along), bias_sum + fold_rows(back))

    def norm_step(block, sums):
        main_sums, rest_sums = sums
        for part in range(TALL // 64):
            start = block * TALL + part * 64
            pairs = []
            for base in (0, half):
                plain, along, main_sums = norm_part(chunk(start, base), main, main_sums)
                pairs.append([plain, along])
            plain, along, rest_sums = norm_part(chunk(start, frames), rest, rest_sums)
            for item, values in enumerate((plain, along)):
                pairs[0][item] = pairs[0][item] + jnp.where(low, values, 0.0)
                pairs[1][item] = pairs[1][item] + jnp.where(low, 0.0, values)
            for (plain, along), base in zip(pairs, (0, half)):
                columns_s[chunk(start, base)] = jnp.where(
                    lane == 0,
                    jnp.sum(plain, axis=-1, keepdims=True),
                    jnp.where(lane == 1, jnp.sum(along, axis=-1, keepdims=True), 0.0),
                )
        return main_sums, rest_sums

    (main_gain, main_bias), (rest_gain, rest_bias) = lax.fori_loop(
        0, half // TALL, norm_step, ((zero, zero), (zero, zero)), unroll=2
    )
    grad_out.go()
    rate_out.go()
    totals = jnp.concatenate(
        [jnp.transpose(columns_s[block * BLOCK : (block + 1) * BLOCK])[:2] for block in range(blocks)], axis=0
    )
    high = totals.astype(BF16)
    low_part = (totals - high.astype(F32)).astype(BF16)
    for block in range(blocks):
        mixed_out.buffer[block, BLOCK:, :LANES] = high
        mixed_out.buffer[block, BLOCK:, LANES:] = low_part
    mixed_out.go(slice(None), pl.ds(BLOCK, 2 * blocks))

    def vectors(part, lines):
        taps = jnp.sum(tap_sum_s[part], axis=1)[:KERNEL]
        stacked = jnp.concatenate([taps] + [one_row(line) for line in lines], axis=0)
        if part:
            stacked = stacked + turn(stacked)
        return jnp.transpose(
            jnp.concatenate([stacked, jnp.zeros((LANES - stacked.shape[0], LANES), F32)], axis=0)
        )

    vectors_out[:LANES] = vectors(0, (main_conv, main_gain, main_bias, main_up))
    vectors_out[LANES:] = vectors(1, (rest_conv, rest_gain, rest_bias, rest_up))[: channels - LANES]


def attend_back_kernel(
    cot_ref,
    merge_ref,
    head_ref,
    attn_ref,
    value_ref,
    prob_ref,
    key_ref,
    coarse_ref,
    fine_ref,
    pos_ref,
    query_ref,
    n_ref,
    q_position_ref,
    qkv_ref,
    hat_ref,
    gain_ref,
    early_ref,
    branch_out,
    total_out,
    pack_0,
    pack_1,
    pack_2,
    pack_3,
    lines_out,
    grad_s,
    raw_s,
    projected_s,
    parts_s,
    grads_s,
):
    place = lax.axis_index("tm")
    frames = raw_s.shape[0]
    blocks = frames // BLOCK
    half = D // 2
    zero = jnp.zeros((8, LANES), F32)
    cot_ref, merge_ref, head_ref, attn_ref = cot_ref(), merge_ref(), head_ref(), attn_ref()
    head_ref[HEAD:] = jnp.zeros((LANES - HEAD, D), BF16)
    begin(value_ref, prob_ref, key_ref, pos_ref)

    @pl.loop(0, frames // TALL, unroll=4)
    def _(block):
        rows = rows_of(block, TALL)
        branch = dot_nt(cot_ref[rows], merge_ref[...]).astype(BF16)
        branch_out.buffer[rows] = branch
        grad_s[rows] = (dot_nt(branch, head_ref[...]) * attn_ref[rows, HEAD : HEAD + 1]).astype(BF16)

    branch_out.go()
    value_ref, prob_ref = value_ref(), prob_ref()
    key_ref, pos_ref = key_ref(), pos_ref()
    begin(query_ref, n_ref, q_position_ref, qkv_ref, hat_ref, early_ref)

    def score_step(block, sums):
        content_sum, position_sum = sums
        rows = rows_of(block, TALL)
        grad = grad_s[rows]
        score = dot_nt(grad, value_ref[...])
        for part in range(TALL // 32):
            at = pl.ds(pl.multiple_of(block * TALL + part * 32, 32), 32)
            inner = slice(part * 32, part * 32 + 32)
            delta = jnp.sum(grad[inner].astype(F32) * attn_ref[at], axis=1, keepdims=True)
            raw_s[at] = (prob_ref[at].astype(F32) * (score[inner] - delta)).astype(BF16)
        query = dot_nn(raw_s[rows], key_ref[...]) * 0.125
        for part in range(TALL // 32):
            at = pl.ds(pl.multiple_of(block * TALL + part * 32, 32), 32)
            inner = part * 32 % BLOCK
            sine, cosine = angle_rows(
                coarse_ref, fine_ref, block * (TALL // BLOCK) + part * 32 // BLOCK, slice(inner, inner + 32)
            )
            inner = slice(part * 32, part * 32 + 32)
            first, second = query[inner, LANES : LANES + half], query[inner, LANES + half :]
            projected_s[at, :half] = (first * sine - second * cosine).astype(BF16)
            projected_s[at, half:] = (first * cosine + second * sine).astype(BF16)
        position = dot_nn(projected_s[rows], pos_ref[...])
        content = query[:, :LANES]
        parts_s[rows, :LANES] = (content + position).astype(BF16)
        return content_sum + fold_rows(content), position_sum + fold_rows(position)

    content_sum, position_sum = lax.fori_loop(0, frames // TALL, score_step, (zero, zero), unroll=4)
    query_ref, n_ref, q_position_ref = query_ref(), n_ref(), q_position_ref()
    qkv_ref, hat_ref = qkv_ref(), hat_ref()
    grad_key = dot_tn(query_ref[...], raw_s[...])
    grad_value = dot_tn(grad_s[...], prob_ref[...])
    for block in range(blocks):
        at = slice(block * BLOCK, (block + 1) * BLOCK)
        parts_s[at, LANES : 2 * LANES] = jnp.transpose(grad_key[:, at]).astype(BF16)
        parts_s[at, 2 * LANES :] = jnp.transpose(grad_value[:, at]).astype(BF16)
    grads_s[:HEAD] = dot_tn(parts_s[:, :LANES], n_ref[...])[:HEAD]
    grads_s[HEAD : 2 * HEAD] = dot_nn(grad_key.astype(BF16), n_ref[...])[:HEAD]
    grads_s[2 * HEAD : 3 * HEAD] = dot_nn(grad_value.astype(BF16), n_ref[...])[:HEAD]
    grads_s[3 * HEAD :] = dot_tn(q_position_ref[...], projected_s[...])[:HEAD]
    stream = lax.axis_index("stream")
    early_ref = early_ref()
    for apart, pack_out in enumerate((pack_0, pack_1, pack_2, pack_3)):
        quarter = lax.bitwise_xor(stream, jnp.int32(apart))
        lanes = pl.ds(pl.multiple_of(quarter * LANES, LANES), LANES)
        pack_out.buffer[: 4 * HEAD] = grads_s[:, lanes].astype(BF16)
        pack_out.buffer[4 * HEAD :] = early_ref[quarter]
        pack_out.go()
    gain = line_of(gain_ref)
    wide_zero = jnp.zeros((8, D), F32)

    def norm_step(block, sums):
        gain_sum, bias_sum = sums
        grad = dot_nt(parts_s[rows_of(block, TALL)], qkv_ref[...])
        for part in range(TALL // 32):
            at = pl.ds(pl.multiple_of(block * TALL + part * 32, 32), 32)
            own = grad[part * 32 : part * 32 + 32]
            total_out.buffer[at] = (own * gain).astype(BF16)
            gain_sum = gain_sum + fold_rows(own * hat_ref[at].astype(F32))
            bias_sum = bias_sum + fold_rows(own)
        return gain_sum, bias_sum

    gain_sum, bias_sum = lax.fori_loop(0, frames // TALL, norm_step, (wide_zero, wide_zero), unroll=4)
    lane = lax.broadcasted_iota(jnp.int32, (1, LANES), 1)

    def own_lanes(sums):
        line = one_row(sums)
        line = line + turn(line)
        tiles = [
            jnp.where(lax.div(tile * LANES + lane, HEAD) == place, line, 0.0) for tile in range(D // LANES)
        ]
        return jnp.concatenate(tiles, axis=1)

    lines_out[...] = jnp.concatenate(
        [
            one_row(gain_sum),
            one_row(bias_sum),
            own_lanes(content_sum),
            own_lanes(position_sum),
            jnp.zeros((4, D), F32),
        ],
        axis=0,
    )


def mlp_second_kernel(
    mixed_ref,
    gate_pre_ref,
    grad_ref,
    rate_ref,
    hat_ref,
    up_ref,
    norm_hat_ref,
    gain_ref,
    other_ref,
    n_ref,
    vectors_ref,
    first_lines_ref,
    head_lines_ref,
    total_out,
    pack_0,
    pack_1,
    pack_2,
    pack_3,
    pre_s,
    columns_s,
    grad_up_s,
    lines_s,
    up_columns_s,
):
    packs = (pack_0, pack_1, pack_2, pack_3)
    stream = lax.axis_index("stream")
    place = lax.axis_index("tm")
    frames = pre_s.shape[0]
    half = frames // 2
    blocks = frames // BLOCK
    quarters = len(packs)
    channels = vectors_ref.shape[0]
    share = channels // quarters
    totals = jnp.zeros((2 * blocks, LANES), F32)
    mixed_ref = mixed_ref()
    for source in range(mixed_ref.shape[0]):
        both = mixed_ref[source].astype(F32)
        totals = totals + (both[:, :LANES] + both[:, LANES:])
    totals = totals * (1.0 / HALF)
    columns = jnp.transpose(jnp.concatenate([totals, jnp.zeros((LANES - 2 * blocks, LANES), F32)], axis=0))
    lane = lax.broadcasted_iota(jnp.int32, (BLOCK, LANES), 1)
    for block in range(blocks):
        columns_s[block * BLOCK : (block + 1) * BLOCK] = jnp.where(
            lane == 0, columns[:, 2 * block : 2 * block + 1], columns[:, 2 * block + 1 : 2 * block + 2]
        )
    gate_pre_ref, grad_ref, rate_ref, hat_ref = gate_pre_ref(), grad_ref(), rate_ref(), hat_ref()
    begin(n_ref, up_ref, norm_hat_ref, other_ref)
    low = low_lanes(64)
    gain = line_of(gain_ref)

    def chunk(start, base=0):
        return pl.ds(pl.multiple_of(start, 64) + base, 64)

    def pre_part(rows, table, up_sum):
        plain, along = table
        hat, rate = hat_ref[rows].astype(F32), rate_ref[rows].astype(F32)
        pre = (grad_ref[rows].astype(F32) - rate * (plain + hat * along)).astype(BF16).astype(F32)
        return pre, up_sum + fold_rows(pre)

    def pre_step(block, sums):
        main_up, rest_up = sums
        for part in range(TALL // 64):
            start = block * TALL + part * 64
            tables = []
            for base in (0, half):
                rows = chunk(start, base)
                values = columns_s[rows]
                table = [values[:, item : item + 1] for item in range(2)]
                tables.append(table)
                pre, main_up = pre_part(rows, table, main_up)
                pre_s[rows, :LANES] = gate_pre_ref[rows]
                pre_s[rows, 2 * LANES :] = pre.astype(BF16)
            rows = chunk(start, frames)
            table = [jnp.where(low, one, other) for one, other in zip(*tables)]
            pre, rest_up = pre_part(rows, table, rest_up)
            gate_pre = gate_pre_ref[rows].astype(F32)
            pre_s[chunk(start), LANES : 2 * LANES] = jnp.where(low, gate_pre, turn(pre)).astype(BF16)
            pre_s[chunk(start, half), LANES : 2 * LANES] = jnp.where(low, turn(gate_pre), pre).astype(BF16)
        return main_up, rest_up

    zero = jnp.zeros((8, LANES), F32)
    main_up, rest_up = lax.fori_loop(0, half // TALL, pre_step, (zero, zero), unroll=2)
    n_ref, up_ref, norm_hat_ref, other_ref = n_ref(), up_ref(), norm_hat_ref(), other_ref()
    grad_up_s[...] = dot_tn(pre_s[:, LANES:], n_ref[...])
    wide_zero = jnp.zeros((8, D), F32)

    def norm_step(block, sums):
        gain_sum, bias_sum = sums
        rows = rows_of(block, BLOCK)
        grad = dot_nt(pre_s[rows], up_ref[...])
        total_out.buffer[block] = (grad * gain + other_ref[rows].astype(F32)).astype(BF16)
        return gain_sum + fold_rows(grad * norm_hat_ref[rows].astype(F32)), bias_sum + fold_rows(grad)

    gain_sum, bias_sum = lax.fori_loop(0, blocks, norm_step, (wide_zero, wide_zero), unroll=4)
    total_out.go()
    rest_line = one_row(rest_up)
    up_columns_s[:LANES] = jnp.transpose(jnp.broadcast_to(one_row(main_up), (LANES, LANES)))
    up_columns_s[LANES:] = jnp.transpose(jnp.broadcast_to(rest_line + turn(rest_line), (LANES, LANES)))[:LOW]
    first_device = (place == 0).astype(F32)
    lines_s[...] = jnp.concatenate(
        [
            head_lines_ref[0:2],
            one_row(gain_sum),
            one_row(bias_sum),
            head_lines_ref[2:4],
            first_lines_ref[0:2] * first_device,
            jnp.zeros((8, D), F32),
        ],
        axis=0,
    )
    gate_at = KERNEL + 3
    lane = lax.broadcasted_iota(jnp.int32, (share, LANES), 1)
    for apart, pack_out in enumerate(packs):
        quarter = lax.bitwise_xor(stream, jnp.int32(apart))
        lanes = pl.ds(pl.multiple_of(quarter * LANES, LANES), LANES)
        pack_out[:LANES] = grad_up_s[LANES:, lanes].astype(BF16)
        pack_out[LANES:channels] = grad_up_s[LOW:LANES, lanes].astype(BF16)
        table = vectors_ref[pl.ds(pl.multiple_of(quarter * share, 8), share)]
        for other in range(2):
            at = pl.ds(pl.multiple_of((2 * lax.rem(quarter, 2) + other) * share, 8), share)
            column = jnp.where(
                quarter < quarters // 2, vectors_ref[at][:, gate_at : gate_at + 1], up_columns_s[at][:, 0:1]
            )
            table = jnp.where(lane == gate_at + other, column, table)
        pack_out[channels : channels + share] = table.astype(BF16)
        pack_out[channels + share :] = lines_s[:, lanes].astype(BF16)


def output_kernel(
    x_ref, mixed_ref, head_ref, down_ref, down_bias_ref, merge_ref, merge_bias_ref, out_ref, joined_out
):
    sources = mixed_ref.shape[0]
    rows = x_ref.shape[0]
    channels = HALF // sources
    share = channels // 4
    attn_parts = []
    branch_attn = jnp.zeros((rows, D), F32)
    branch_mlp = jnp.zeros((rows, D), F32)
    for source in range(sources):
        attn = turn(mixed_ref[source, :rows, LANES:].astype(F32))[:, :HEAD].astype(BF16)
        attn_parts.append(attn)
        branch_attn = branch_attn + dot_nn(attn, head_ref[source * HEAD : (source + 1) * HEAD])
        down = jnp.concatenate(
            [down_ref[(part * sources + source) * share : (part * sources + source + 1) * share] for part in range(4)],
            axis=0,
        )
        branch_mlp = branch_mlp + dot_nn(mixed_ref[source, :rows, :channels], down)
    joined = jnp.concatenate(
        [branch_attn.astype(BF16), (branch_mlp + line_of(down_bias_ref)).astype(BF16)], axis=1
    )
    result = x_ref[...].astype(F32) + dot_nn(joined, merge_ref[...]) + line_of(merge_bias_ref)
    out_ref[...] = result.astype(BF16)
    turned = jnp.transpose(joined.astype(F32))
    heads = jnp.transpose(jnp.concatenate(attn_parts, axis=1).astype(F32))
    merge_share = turned.shape[0] // (4 * sources)
    head_share = heads.shape[0] // (4 * sources)
    used = 4 * (merge_share + head_share)
    for target in range(sources):
        for part in range(4):
            at = (part * sources + target) * merge_share
            joined_out[target, part * merge_share : (part + 1) * merge_share] = turned[
                at : at + merge_share
            ].astype(BF16)
            at = (part * sources + target) * head_share
            to = 4 * merge_share + part * head_share
            joined_out[target, to : to + head_share] = heads[at : at + head_share].astype(BF16)
        joined_out[target, used:] = jnp.zeros((joined_out.shape[1] - used, rows), BF16)


def merge_kernel(joined_ref, branch_ref, cot_ref, pack_0, pack_1, pack_2, pack_3, merge_s, head_s):
    stream = lax.axis_index("stream")
    cot_ref = cot_ref()
    sources, _, rows = joined_ref.shape
    merge_rows = 2 * D // sources
    head_rows = D // sources
    grad_merge = jnp.zeros((merge_rows, D), F32)
    grad_head = jnp.zeros((head_rows, D), F32)
    for source in range(sources):
        at = slice(source * rows, (source + 1) * rows)
        joined = joined_ref[source]
        grad_merge = grad_merge + dot_nn(joined[:merge_rows], cot_ref[at])
        grad_head = grad_head + dot_nn(joined[merge_rows : merge_rows + head_rows], branch_ref[at])
    merge_s[...] = grad_merge
    head_s[...] = grad_head
    for apart, pack_out in enumerate((pack_0, pack_1, pack_2, pack_3)):
        pack_out = pack_out.buffer
        quarter = lax.bitwise_xor(stream, jnp.int32(apart))
        for grad_s, base in ((merge_s, 0), (head_s, merge_rows)):
            share = grad_s.shape[0] // 4
            at = pl.ds(pl.multiple_of(quarter * share, share), share)
            for tile in range(4):
                to = base + tile * share
                pack_out[to : to + share] = grad_s[at, tile * LANES : (tile + 1) * LANES].astype(BF16)


def frames_kernel(x_ref, cot_ref, total_ref, out_ref):
    for part in range(x_ref.shape[0] // 32):
        rows = slice(part * 32, part * 32 + 32)
        inputs = x_ref[rows].astype(F32)
        mean = jnp.mean(inputs, axis=-1, keepdims=True)
        centred = inputs - mean
        rate = lax.rsqrt(jnp.mean(centred * centred, axis=-1, keepdims=True) + EPS)
        hat = centred * rate
        grad = total_ref[0, rows].astype(F32)
        for source in range(1, total_ref.shape[0]):
            grad = grad + total_ref[source, rows].astype(F32)
        plain = jnp.mean(grad, axis=-1, keepdims=True)
        along = jnp.mean(grad * hat, axis=-1, keepdims=True)
        out_ref[rows] = cot_ref[rows].astype(F32) + rate * (grad - plain - hat * along)


def add_kernel(*refs):
    out_ref = refs[-1]
    first = 0
    for at in range(0, len(refs) - 1, 4):
        total = refs[at][...].astype(F32)
        for ref in refs[at + 1 : at + 4]:
            total = total + ref[...].astype(F32)
        out_ref[first : first + total.shape[0]] = total.astype(BF16)
        first += total.shape[0]


def gather_parts(near_ref, far_ref, all_s):
    place = lax.axis_index("tm")
    for apart in range(all_s.shape[0]):
        part_ref = far_ref if apart % 2 else near_ref
        all_s[lax.bitwise_xor(jnp.int32(apart), place)] = part_ref[apart // 2]


def lines_from(all_s, base, size):
    return jnp.concatenate([all_s[source, base : base + size] for source in range(all_s.shape[0])], axis=0).astype(F32)


def early_kernel(near_ref, far_ref, qkv_out, pos_out, down_out, up_out, all_s):
    gather_parts(near_ref, far_ref, all_s)
    sources = all_s.shape[0]
    share = HALF // (4 * sources)
    for kind in range(4):
        lines = jnp.transpose(lines_from(all_s, kind * HEAD, HEAD))
        if kind < 3:
            qkv_out[:, kind * D : (kind + 1) * D] = lines
        else:
            pos_out[...] = lines
    base = 4 * HEAD
    for source in range(sources):
        for tile in range(4):
            down_out[source * share : (source + 1) * share, tile * LANES : (tile + 1) * LANES] = all_s[
                source, base + tile * share : base + (tile + 1) * share
            ].astype(F32)
    wide = sources * share
    for group in range(4):
        up_out.buffer[:, group * wide : (group + 1) * wide] = jnp.transpose(
            lines_from(all_s, base + 4 * share + group * share, share)
        )


def late_kernel(*refs):
    _, near_ref, far_ref = refs[:3]
    (
        attn_gain_out,
        attn_bias_out,
        mlp_gain_out,
        mlp_bias_out,
        content_out,
        position_out,
        outw_out,
        up_out,
        up_bias_out,
        gain_out,
        bias_out,
        taps_out,
        conv_bias_out,
        down_bias_out,
        merge_out,
        merge_bias_out,
        all_s,
    ) = refs[3:]
    gather_parts(near_ref, far_ref, all_s)
    sources = all_s.shape[0]
    channels = HALF // sources
    share = channels // 4
    base = 0
    for group in range(4):
        at = group * sources * share
        up_out.buffer[:, at : at + sources * share] = jnp.transpose(lines_from(all_s, base + group * share, share))
    up_out.go()
    table = jnp.transpose(lines_from(all_s, base + channels, share))
    taps_out[...] = table[:KERNEL]
    conv_bias_out[...] = table[KERNEL]
    gain_out[...] = table[KERNEL + 1]
    bias_out[...] = table[KERNEL + 2]
    wide = sources * share
    up_bias_out[:wide] = table[KERNEL + 3]
    up_bias_out[wide:] = table[KERNEL + 4]
    base = base + channels + share
    lines = all_s[0, base : base + 16].astype(F32)
    for source in range(1, sources):
        lines = lines + all_s[source, base : base + 16].astype(F32)
    outs = (attn_gain_out, attn_bias_out, mlp_gain_out, mlp_bias_out, content_out, position_out, down_bias_out, merge_bias_out)
    for line, out in enumerate(outs):
        out[...] = lines[line]
    base = base + 16
    merge_share = 2 * D // (4 * sources)
    head_share = D // (4 * sources)
    for source in range(sources):
        for tile in range(4):
            lanes = slice(tile * LANES, (tile + 1) * LANES)
            at = base + tile * merge_share
            merge_out[source * merge_share : (source + 1) * merge_share, lanes] = all_s[
                source, at : at + merge_share
            ].astype(F32)
            at = base + 4 * merge_share + tile * head_share
            outw_out[source * head_share : (source + 1) * head_share, lanes] = all_s[
                source, at : at + head_share
            ].astype(F32)


def moved(block, axis, bits):
    count = lax.axis_size(axis)
    return lax.ppermute(block, axis, [(index, index ^ bits) for index in range(count)])


def over_streams(packs):
    return [packs[0]] + [moved(packs[bits], "stream", bits) for bits in range(1, lax.axis_size("stream"))]


def near_blocks(block):
    return [block] + [moved(block, "tm", bits) for bits in range(2, lax.axis_size("tm"), 2)]


def far_blocks(near):
    far = [moved(part, "tm", 1) for part in near]
    return [part for pair in zip(near, far) for part in pair]


def far_stack(near):
    stack = jnp.stack(near)
    return stack, moved(stack, "tm", 1)


def head_device(
    frames,
    lengths,
    cotangent,
    ln_attn_gain,
    ln_attn_bias,
    ln_mlp_gain,
    ln_mlp_bias,
    qkv_weight,
    content_bias,
    position_bias,
    pos_weight,
    out_weight,
    up_weight,
    up_bias,
    gate_norm_gain,
    gate_norm_bias,
    conv_kernel,
    conv_bias,
    down_weight,
    down_bias,
    merge_weight,
    merge_bias,
):
    count = lax.axis_size("tm")
    quarters = lax.axis_size("stream")
    own = frames.shape[1]
    total = own * count
    folded = total + total // 2
    padded = folded + 4 * MARGIN
    share = HALF // (quarters * count)
    channels = HALF // count
    quarter = D // quarters
    own_frames = frames[0]
    own_cotangent = cotangent[0]

    whole, late = Part(), Part(late=True)
    near = near_blocks(own_frames)
    cot_near = near_blocks(own_cotangent)
    up_own, table, qkv_own, pos_own, bias_own = kernel_call(
        select_kernel,
        [
            ((D, 3 * LANES), BF16),
            ((2, 8 + KERNEL + 1, LANES), F32),
            ((D, 3 * LANES), BF16),
            ((D, LANES), BF16),
            ((8, LANES), F32),
        ],
        10 * "v",
    )(
        up_weight,
        up_bias,
        gate_norm_gain,
        gate_norm_bias,
        conv_bias,
        conv_kernel,
        qkv_weight,
        pos_weight,
        content_bias,
        position_bias,
    )
    near, up_own = lax.optimization_barrier((near, up_own))
    blocks = far_blocks(near)
    frequency = jnp.exp(jnp.arange(D // 2, dtype=F32) * (-2.0 * math.log(10000.0) / D))
    coarse = jnp.arange(0, total, BLOCK, dtype=F32)[:, None] * frequency[None]
    fine = jnp.arange(BLOCK, dtype=F32)[:, None] * frequency[None]
    coarse_table = jnp.concatenate([jnp.sin(coarse), jnp.cos(coarse)], axis=1)
    fine_table = jnp.concatenate([jnp.sin(fine), jnp.cos(fine)], axis=1)

    n_attn, n_mlp, hat, q_position, query, key, value, prob, attn, stats = kernel_call(
        attend_kernel,
        [
            ((total, D), BF16, 1),
            ((total, D), BF16, 1),
            ((total, D), BF16, 1),
            ((total, LANES), BF16, 1),
            ((total, LANES + D), BF16, 1),
            ((total, LANES + D), BF16, 1),
            ((total, LANES), BF16, 1),
            ((total, total), BF16, 1),
            ((total, LANES), F32, 1),
            ((total, LANES), F32, 1),
        ],
        [
            "s",
            blocks_part(),
            *"vvvvvvvvv",
            Part((D, HALF), lambda refs, buffer: [(refs[0].at[:, pl.ds(HALF, HALF)], buffer)], late=True),
            "v",
        ],
        bounds=True,
    )(
        lengths,
        *blocks,
        ln_attn_gain,
        ln_attn_bias,
        ln_mlp_gain,
        ln_mlp_bias,
        qkv_own,
        pos_own,
        bias_own,
        coarse_table,
        fine_table,
        up_weight,
        up_bias,
    )

    n_mlp, cot_near = lax.optimization_barrier((n_mlp, cot_near))
    cot = far_blocks(cot_near)

    def own_down(refs, buffer):
        place = lax.axis_index("tm")
        stride = HALF // quarters
        return [
            (
                refs[0].at[pl.ds(pl.multiple_of(part * stride + share * place, 16), share)],
                buffer.at[pl.ds(part * share, share)],
            )
            for part in range(quarters)
        ]

    mixed, gate_pre, grad_y, slope, gate_hat, early_pack, vectors, first_lines = kernel_call(
        mlp_first_kernel,
        [
            ((count, own + 16, 2 * LANES), BF16, 1),
            ((folded, LANES), BF16, 1),
            ((folded, LANES), BF16, 1),
            ((folded, LANES), BF16, 1),
            ((folded, LANES), BF16, 1),
            ((quarters, 8 * share, LANES), BF16, 1),
            ((channels, LANES), F32),
            ((8, D), F32),
        ],
        [
            "s",
            whole,
            "v",
            "v",
            whole,
            blocks_part(late=True),
            rows_part(D, D, late=True),
            Part((2 * LANES, D), own_down, late=True),
            Part(late=True),
        ],
        [
            ((folded, LANES), F32),
            ((folded, LANES), F32),
            ((total, 2 * LANES), BF16),
            ((folded, LANES), F32),
            ((folded, LANES), F32),
            ((padded, LANES), F32),
            ((padded, LANES), F32),
            ((folded, LANES), F32),
            ((folded, LANES), F32),
            ((total, D), BF16),
            ((total, 2 * LANES), BF16),
            ((2, 32, 8, LANES), F32),
            ((2, 32, 8, LANES), F32),
            ((2, 32, 8, LANES), F32),
            ((total, LANES), F32),
            ((3, WINDOW + 2 * MARGIN, LANES), F32),
            ((3, WINDOW + 2 * MARGIN, LANES), F32),
        ],
        bounds=True,
    )(lengths, n_mlp, up_own, table, stats, *cot, merge_weight, down_weight, attn)
    mixed_own = lax.all_to_all(mixed, "tm", 0, 0, tiled=True)

    def own_head(refs, buffer):
        at = pl.ds(pl.multiple_of(lax.axis_index("tm") * HEAD, HEAD), HEAD)
        return [(refs[0].at[at], buffer.at[pl.ds(0, HEAD)])]

    branch, from_attn, *head_packs, head_lines = kernel_call(
        attend_back_kernel,
        [
            ((total, D), BF16, 1),
            ((total, D), BF16, 1),
            *([((4 * HEAD + 8 * share, LANES), BF16, 1)] * quarters),
            ((8, D), F32),
        ],
        [
            blocks_part(),
            rows_part(0, D),
            Part((LANES, D), own_head),
            whole,
            late,
            late,
            late,
            "v",
            "v",
            late,
            Part((total, LANES), lambda refs, buffer: [(refs[0].at[:, pl.ds(0, LANES)], buffer)], late=True),
            late,
            late,
            late,
            late,
            "v",
            late,
        ],
        [
            ((total, LANES), BF16),
            ((total, total), BF16),
            ((total, D), BF16),
            ((total, 3 * LANES), BF16),
            ((4 * HEAD, D), F32),
        ],
    )(
        *cot,
        merge_weight,
        out_weight,
        attn,
        value,
        prob,
        key,
        coarse_table,
        fine_table,
        pos_own,
        query,
        n_attn,
        q_position,
        qkv_own,
        hat,
        ln_attn_gain,
        early_pack,
    )
    head_parts = over_streams(head_packs)
    mixed_own, _ = lax.optimization_barrier((mixed_own, head_lines))
    out_rows, joined = kernel_call(
        output_kernel,
        [((own, D), BF16), ((count, 256, own), BF16)],
        "vvvvvvv",
        megas=24,
    )(own_frames, mixed_own, out_weight, down_weight, down_bias, merge_weight, merge_bias)
    joined_all = lax.all_to_all(joined, "tm", 0, 0, tiled=True)
    gate_pre, _ = lax.optimization_barrier((gate_pre, joined))
    up_rows = 5 * share + 16
    from_both, *up_packs = kernel_call(
        mlp_second_kernel,
        [((count, own, D), BF16, 1)] + [((up_rows, LANES), BF16)] * quarters,
        [
            Part(
                (count, 2 * total // BLOCK, 2 * LANES),
                lambda refs, buffer: [(refs[0].at[:, pl.ds(own, 2 * total // BLOCK)], buffer)],
            ),
            *([whole] * 4),
            late,
            late,
            "v",
            late,
            late,
            *"vvv",
        ],
        [
            ((total, 3 * LANES), BF16),
            ((total, LANES), F32),
            ((2 * LANES, D), F32),
            ((16, D), F32),
            ((channels, LANES), F32),
        ],
    )(
        mixed_own,
        gate_pre,
        grad_y,
        slope,
        gate_hat,
        up_own,
        hat,
        ln_mlp_gain,
        from_attn,
        n_mlp,
        vectors,
        first_lines,
        head_lines,
    )
    up_parts = over_streams(up_packs)
    head_parts, up_parts[1] = lax.optimization_barrier((head_parts, up_parts[1]))
    (early_part,) = kernel_call(add_kernel, [((4 * HEAD + 8 * share, LANES), BF16)], quarters * "v", megas=24)(
        *head_parts
    )
    early_near = near_blocks(early_part)
    from_all = lax.all_to_all(from_both, "tm", 0, 0, tiled=True)
    joined_all, up_parts, early_near = lax.optimization_barrier((joined_all, up_parts, early_near))
    merge_rows = 3 * D // count
    merge_packs = kernel_call(
        merge_kernel,
        [((merge_rows, LANES), BF16, 1)] * quarters,
        ["f", "f", blocks_part()],
        [((2 * D // count, D), F32), ((D // count, D), F32)],
    )(joined_all, branch, *cot)
    merge_parts = over_streams(merge_packs)
    early_near, _ = lax.optimization_barrier((early_near, merge_packs[0]))
    early_all = far_stack(early_near)
    (grad_frames,) = kernel_call(frames_kernel, [((own, D), F32)], "vvv", megas=24)(
        own_frames, own_cotangent, from_all
    )
    grad_qkv, grad_pos, grad_down, half_up = kernel_call(
        early_kernel,
        [
            ((quarter, 3 * D), F32),
            ((quarter, D), F32),
            ((HALF // quarters, D), F32),
            ((quarter, 2 * HALF), F32, 1, (quarter, HALF), lambda ref: ref.at[:, pl.ds(0, HALF)]),
        ],
        "vv",
        [((count, 4 * HEAD + 8 * share, LANES), BF16)],
        megas=24,
    )(*early_all)
    merge_parts, grad_pos = lax.optimization_barrier((merge_parts, grad_pos))
    late_rows = up_rows + merge_rows
    (late_part,) = kernel_call(add_kernel, [((late_rows, LANES), BF16)], 2 * quarters * "v", megas=24)(
        *up_parts, *merge_parts
    )
    late_near = near_blocks(late_part)
    late_near, grad_frames = lax.optimization_barrier((late_near, grad_frames))
    late_parts = far_stack(late_near)
    late = kernel_call(
        late_kernel,
        [((quarter,), F32)] * 6
        + [
            ((quarter, D), F32),
            ((quarter, 2 * HALF), F32, 1, (quarter, HALF), lambda ref: ref.at[:, pl.ds(HALF, HALF)]),
            ((2 * HALF // quarters,), F32),
            ((HALF // quarters,), F32),
            ((HALF // quarters,), F32),
            ((KERNEL, HALF // quarters), F32),
            ((HALF // quarters,), F32),
            ((quarter,), F32),
            ((2 * D // quarters, D), F32),
            ((quarter,), F32),
        ],
        "kvv",
        [((count,) + late_part.shape, BF16)],
        megas=24,
        aliases={0: 7},
    )(half_up, *late_parts)
    return (
        out_rows[None],
        grad_frames[None],
        *late[:4],
        grad_qkv,
        *late[4:6],
        grad_pos,
        *late[6:13],
        grad_down,
        *late[13:],
    )


def per_device(*operands):
    fits = (
        lax.axis_size("tm") == HEADS
        and lax.axis_size("stream") * LANES == D
        and operands[0].shape[1] == BLOCK
    )
    return head_device(*operands) if fits else frame_device(*operands)


def solution(mesh):
    return jax.shard_map(
        per_device,
        mesh=mesh,
        in_specs=(
            P("stream", "tm", None),
            P("stream", None),
            P("stream", "tm", None),
            P(),
            P(),
            P(),
            P(),
            P(),
            P(),
            P(),
            P(),
            P(),
            P(),
            P(),
            P(),
            P(),
            P(),
            P(),
            P(),
            P(),
            P(),
            P(),
        ),
        out_specs=(
            P("stream", "tm", None),
            P("stream", "tm", None),
            P("stream"),
            P("stream"),
            P("stream"),
            P("stream"),
            P("stream", None),
            P("stream"),
            P("stream"),
            P("stream", None),
            P("stream", None),
            P("stream", None),
            P("stream"),
            P("stream"),
            P("stream"),
            P(None, "stream"),
            P("stream"),
            P("stream", None),
            P("stream"),
            P("stream", None),
            P("stream"),
        ),
        check_vma=False,
    )
```

```python
import math

import jax
import jax.numpy as jnp
from jax import lax
from jax.experimental import pallas as pl
from jax.experimental.pallas import tpu as pltpu
from jax.sharding import PartitionSpec as P

D = 512
HEADS = 8
HEAD = 64
KERNEL = 31
ITEMS = 5
HALF = 1536


EPS = 1e-05
MASKED = -1e30


def extended(block, sides, width):
    for axis, dim in sides:
        count = lax.axis_size(axis)
        forward = [(i, i + 1) for i in range(count - 1)]
        backward = [(target, source) for source, target in forward]
        low = lax.ppermute(
            lax.slice_in_dim(block, block.shape[dim] - width, None, axis=dim), axis, forward
        )
        high = lax.ppermute(lax.slice_in_dim(block, 0, width, axis=dim), axis, backward)
        block = jnp.concatenate([low, block, high], axis=dim)
    return block


def norm_rows(inputs, scale_row, shift_row):
    row_mean = jnp.mean(inputs, axis=-1, keepdims=True)
    centred = inputs - row_mean
    spread = jnp.mean(centred * centred, axis=-1, keepdims=True)
    return centred * lax.rsqrt(spread + EPS) * scale_row + shift_row


def gelu_exact(inputs):
    return jax.nn.gelu(inputs, approximate=False)


def frame_info(lengths, offset, extent):
    item_ends = jnp.cumsum(lengths)
    first_table = jnp.concatenate([item_ends - lengths, item_ends[-1:]])
    frame_index = offset + jnp.arange(extent, dtype=jnp.int32)
    item_of = jnp.sum((frame_index[:, None] >= item_ends[None, :]).astype(jnp.int32), axis=1)
    labels = jnp.arange(ITEMS + 1, dtype=jnp.int32)
    first_frame = jnp.sum(
        jnp.where(item_of[:, None] == labels[None, :], first_table[None, :], 0), axis=1
    )
    return (frame_index, item_of, frame_index - first_frame)


def angles(place_in):
    frequency = jnp.exp(jnp.arange(D // 2, dtype=jnp.float32) * (-2.0 * math.log(10000.0) / D))
    phase_angle = place_in.astype(jnp.float32)[:, None] * frequency[None, :]
    return (jnp.sin(phase_angle), jnp.cos(phase_angle))


def rel_query(projected, sine_rows, cosine_rows):
    half_size = projected.shape[-1] // 2
    first_half = projected[..., :half_size]
    second_half = projected[..., half_size:]
    sine_wide = sine_rows[:, None, :]
    cosine_wide = cosine_rows[:, None, :]
    return jnp.concatenate(
        [
            first_half * sine_wide + second_half * cosine_wide,
            second_half * sine_wide - first_half * cosine_wide,
        ],
        axis=-1,
    )


def step_size(extent):
    return math.gcd(extent, 512)


def score_block(q_content, q_rel, query_item, query_frame, key_block, key_start, lengths):
    extent = key_block.shape[0]
    key_frame, key_item, key_place = frame_info(lengths, key_start, extent)
    sine_rows, cosine_rows = angles(key_place)
    k_rel = jnp.concatenate([cosine_rows, sine_rows], axis=1).astype(jnp.bfloat16)
    raw_scores = jnp.einsum(
        "qhe,khe->hqk",
        q_content,
        key_block.reshape(extent, HEADS, HEAD),
        preferred_element_type=jnp.float32,
    )
    raw_scores = raw_scores + jnp.einsum(
        "qhc,kc->hqk", q_rel, k_rel, preferred_element_type=jnp.float32
    )
    allowed = (query_item[:, None] == key_item[None, :]) & (
        (query_item[:, None] < ITEMS) | (query_frame[:, None] == key_frame[None, :])
    )
    return (raw_scores, allowed, k_rel)


def block_grads(
    q_content,
    q_rel,
    query_item,
    query_frame,
    grad_out,
    log_total,
    delta_rows,
    key_block,
    value_block,
    key_start,
    lengths,
):
    extent = key_block.shape[0]
    raw_scores, allowed, k_rel = score_block(
        q_content, q_rel, query_item, query_frame, key_block, key_start, lengths
    )
    prob_rows = jnp.where(allowed[None], jnp.exp(raw_scores * 0.125 - log_total[:, :, None]), 0.0)
    grad_prob = jnp.einsum(
        "qhe,khe->hqk",
        grad_out,
        value_block.reshape(extent, HEADS, HEAD),
        preferred_element_type=jnp.float32,
    )
    grad_raw = (prob_rows * (grad_prob - delta_rows[:, :, None]) * 0.125).astype(jnp.bfloat16)
    return (prob_rows.astype(jnp.bfloat16), grad_raw, k_rel)


def frame_device(
    frames,
    lengths,
    cotangent,
    ln_attn_gain,
    ln_attn_bias,
    ln_mlp_gain,
    ln_mlp_bias,
    qkv_weight,
    content_bias,
    position_bias,
    pos_weight,
    out_weight,
    up_weight,
    up_bias,
    gate_norm_gain,
    gate_norm_bias,
    conv_kernel,
    conv_bias,
    down_weight,
    down_bias,
    merge_weight,
    merge_bias,
):
    row_count = frames.shape[1]
    cycle_size = lax.axis_size("tm")
    offset = lax.axis_index("tm") * row_count
    stream_lengths = lengths[0]
    inputs = frames[0].astype(jnp.float32)
    frame_index, item_of, place_in = frame_info(stream_lengths, offset, row_count)
    sine_rows, cosine_rows = angles(place_in)
    attn_norm, attn_pull = jax.vjp(
        norm_rows, inputs, ln_attn_gain.astype(jnp.float32), ln_attn_bias.astype(jnp.float32)
    )
    mlp_norm, mlp_pull = jax.vjp(
        norm_rows, inputs, ln_mlp_gain.astype(jnp.float32), ln_mlp_bias.astype(jnp.float32)
    )
    attn_norm_low = attn_norm.astype(jnp.bfloat16)
    mlp_norm_low = mlp_norm.astype(jnp.bfloat16)
    qkv_rows = jnp.dot(attn_norm_low, qkv_weight, preferred_element_type=jnp.float32)
    query_rows = qkv_rows[:, :D]
    key_rows = qkv_rows[:, D : 2 * D].astype(jnp.bfloat16)
    value_rows = qkv_rows[:, 2 * D :].astype(jnp.bfloat16)
    q_content = (query_rows + content_bias.astype(jnp.float32)).astype(jnp.bfloat16)
    q_position = (query_rows + position_bias.astype(jnp.float32)).astype(jnp.bfloat16)
    content_heads = q_content.reshape(row_count, HEADS, HEAD)
    position_heads = q_position.reshape(row_count, HEADS, HEAD)
    pos_heads = pos_weight.reshape(D, HEADS, HEAD)
    projected = jnp.einsum(
        "the,che->thc", position_heads, pos_heads, preferred_element_type=jnp.float32
    )
    q_rel = rel_query(projected, sine_rows, cosine_rows).astype(jnp.bfloat16)
    start_state = (
        jnp.full((HEADS, row_count), MASKED, jnp.float32),
        jnp.zeros((HEADS, row_count), jnp.float32),
        jnp.zeros((HEADS, row_count, HEAD), jnp.float32),
    )
    fold_state = start_state
    key_piece = lax.all_gather(key_rows, "tm", axis=0, tiled=True)
    value_piece = lax.all_gather(value_rows, "tm", axis=0, tiled=True)
    extent = key_piece.shape[0]
    step_rows = step_size(extent)

    def forward_one_step(inner_state, step_index):
        row_top, row_total, row_acc = inner_state
        key_block = lax.dynamic_slice_in_dim(key_piece, step_index * step_rows, step_rows, 0)
        value_block = lax.dynamic_slice_in_dim(value_piece, step_index * step_rows, step_rows, 0)
        raw_scores, allowed, k_rel = score_block(
            content_heads,
            q_rel,
            item_of,
            frame_index,
            key_block,
            step_index * step_rows,
            stream_lengths,
        )
        scaled = jnp.where(allowed[None], raw_scores * 0.125, MASKED)
        new_top = jnp.maximum(row_top, jnp.max(scaled, axis=2))
        weight = jnp.where(allowed[None], jnp.exp(scaled - new_top[:, :, None]), 0.0)
        factor = jnp.exp(row_top - new_top)
        row_total = row_total * factor + jnp.sum(weight, axis=2)
        row_acc = row_acc * factor[:, :, None] + jnp.einsum(
            "hqk,khe->hqe",
            weight.astype(jnp.bfloat16),
            value_block.reshape(step_rows, HEADS, HEAD),
            preferred_element_type=jnp.float32,
        )
        return ((new_top, row_total, row_acc), None)

    fold_state, unused = lax.scan(
        forward_one_step, fold_state, jnp.arange(extent // step_rows, dtype=jnp.int32)
    )
    row_top, row_total, row_acc = fold_state
    attn_heads = row_acc / row_total[:, :, None]
    log_total = row_top + jnp.log(row_total)
    attn_low = jnp.transpose(attn_heads, (1, 0, 2)).reshape(row_count, D).astype(jnp.bfloat16)
    branch_attn = jnp.dot(attn_low, out_weight, preferred_element_type=jnp.float32).astype(
        jnp.bfloat16
    )
    hidden_pre = jnp.dot(
        mlp_norm_low, up_weight, preferred_element_type=jnp.float32
    ) + up_bias.astype(jnp.float32)
    hidden, gelu_pull = jax.vjp(gelu_exact, hidden_pre)
    gate_half = hidden[:, :HALF]
    conv_norm, conv_pull = jax.vjp(
        norm_rows,
        hidden[:, HALF:],
        gate_norm_gain.astype(jnp.float32),
        gate_norm_bias.astype(jnp.float32),
    )
    conv_in = conv_norm.astype(jnp.bfloat16)
    half_width = KERNEL // 2
    conv_wide = extended(conv_in, (("tm", 0),), half_width)
    wide_frame, wide_item, wide_place = frame_info(
        stream_lengths, offset - half_width, row_count + 2 * half_width
    )
    kernel_rows = conv_kernel.astype(jnp.float32)
    conv_out = conv_bias.astype(jnp.float32) + jnp.zeros_like(gate_half)
    for tap_index in range(KERNEL):
        same_item = (wide_item[tap_index : tap_index + row_count] == item_of)[:, None]
        conv_out = (
            conv_out
            + jnp.where(
                same_item, conv_wide[tap_index : tap_index + row_count].astype(jnp.float32), 0.0
            )
            * kernel_rows[tap_index]
        )
    gated_low = (gate_half * conv_out).astype(jnp.bfloat16)
    branch_mlp = (
        jnp.dot(gated_low, down_weight, preferred_element_type=jnp.float32)
        + down_bias.astype(jnp.float32)
    ).astype(jnp.bfloat16)
    joined = jnp.concatenate([branch_attn, branch_mlp], axis=1)
    result = (
        inputs
        + jnp.dot(joined, merge_weight, preferred_element_type=jnp.float32)
        + merge_bias.astype(jnp.float32)
    )
    out_rows = result.astype(jnp.bfloat16)[None]
    grad_low = cotangent[0]
    grad_rows = grad_low.astype(jnp.float32)
    grad_merge_bias = jnp.sum(grad_rows, axis=0)
    grad_merge_weight = jnp.einsum(
        "tc,td->cd", joined, grad_low, preferred_element_type=jnp.float32
    )
    grad_joined = jnp.einsum(
        "td,cd->tc", grad_low, merge_weight, preferred_element_type=jnp.float32
    )
    grad_attn_branch = grad_joined[:, :D].astype(jnp.bfloat16)
    grad_mlp_branch = grad_joined[:, D:].astype(jnp.bfloat16)
    grad_down_weight = jnp.einsum(
        "tc,td->cd", gated_low, grad_mlp_branch, preferred_element_type=jnp.float32
    )
    grad_down_bias = jnp.sum(grad_mlp_branch.astype(jnp.float32), axis=0)
    grad_gated = jnp.einsum(
        "td,cd->tc", grad_mlp_branch, down_weight, preferred_element_type=jnp.float32
    )
    grad_gate_half = grad_gated * conv_out
    grad_conv_out = (grad_gated * gate_half).astype(jnp.bfloat16)
    grad_conv_rows = grad_conv_out.astype(jnp.float32)
    grad_conv_bias = jnp.sum(grad_conv_rows, axis=0)
    grad_wide = extended(grad_conv_out, (("tm", 0),), half_width)
    kernel_list = []
    grad_conv_in = jnp.zeros_like(grad_conv_rows)
    for tap_index in range(KERNEL):
        same_item = (wide_item[tap_index : tap_index + row_count] == item_of)[:, None]
        kernel_list.append(
            jnp.sum(
                jnp.where(
                    same_item, conv_wide[tap_index : tap_index + row_count].astype(jnp.float32), 0.0
                )
                * grad_conv_rows,
                axis=0,
            )
        )
        back_start = 2 * half_width - tap_index
        back_item = (wide_item[back_start : back_start + row_count] == item_of)[:, None]
        grad_conv_in = (
            grad_conv_in
            + jnp.where(
                back_item, grad_wide[back_start : back_start + row_count].astype(jnp.float32), 0.0
            )
            * kernel_rows[tap_index]
        )
    grad_conv_kernel = jnp.stack(kernel_list)
    grad_second, grad_gate_norm_gain, grad_gate_norm_bias = conv_pull(grad_conv_in)
    (grad_pre_rows,) = gelu_pull(jnp.concatenate([grad_gate_half, grad_second], axis=1))
    grad_pre = grad_pre_rows.astype(jnp.bfloat16)
    grad_up_bias = jnp.sum(grad_pre.astype(jnp.float32), axis=0)
    grad_up_weight = jnp.einsum(
        "tc,tf->cf", mlp_norm_low, grad_pre, preferred_element_type=jnp.float32
    )
    grad_mlp_norm = jnp.einsum("tf,cf->tc", grad_pre, up_weight, preferred_element_type=jnp.float32)
    grad_out_weight = jnp.einsum(
        "tc,td->cd", attn_low, grad_attn_branch, preferred_element_type=jnp.float32
    )
    grad_attn_low = jnp.einsum(
        "td,cd->tc", grad_attn_branch, out_weight, preferred_element_type=jnp.float32
    ).astype(jnp.bfloat16)
    grad_out_heads = grad_attn_low.reshape(row_count, HEADS, HEAD)
    delta_rows = jnp.sum(
        jnp.transpose(grad_out_heads.astype(jnp.float32), (1, 0, 2)) * attn_heads, axis=2
    )
    total_frames = row_count * cycle_size
    back_start_state = (
        jnp.zeros((row_count, HEADS, HEAD), jnp.float32),
        jnp.zeros((row_count, HEADS, D), jnp.float32),
        jnp.zeros((total_frames, D), jnp.float32),
        jnp.zeros((total_frames, D), jnp.float32),
    )
    back_key_piece = lax.all_gather(key_rows, "tm", axis=0, tiled=True)
    back_value_piece = lax.all_gather(value_rows, "tm", axis=0, tiled=True)
    extent = back_key_piece.shape[0]
    back_step_rows = step_size(extent)

    def back_one_step(inner_state, step_index):
        grad_content, grad_rel = inner_state
        key_block = lax.dynamic_slice_in_dim(
            back_key_piece, step_index * back_step_rows, back_step_rows, 0
        )
        value_block = lax.dynamic_slice_in_dim(
            back_value_piece, step_index * back_step_rows, back_step_rows, 0
        )
        prob_low, grad_raw, k_rel = block_grads(
            content_heads,
            q_rel,
            item_of,
            frame_index,
            grad_out_heads,
            log_total,
            delta_rows,
            key_block,
            value_block,
            step_index * back_step_rows,
            stream_lengths,
        )
        grad_content = grad_content + jnp.einsum(
            "hqk,khe->qhe",
            grad_raw,
            key_block.reshape(back_step_rows, HEADS, HEAD),
            preferred_element_type=jnp.float32,
        )
        grad_rel = grad_rel + jnp.einsum(
            "hqk,kc->qhc", grad_raw, k_rel, preferred_element_type=jnp.float32
        )
        key_part = jnp.einsum(
            "hqk,qhe->khe", grad_raw, content_heads, preferred_element_type=jnp.float32
        ).reshape(back_step_rows, D)
        value_part = jnp.einsum(
            "hqk,qhe->khe", prob_low, grad_out_heads, preferred_element_type=jnp.float32
        ).reshape(back_step_rows, D)
        return ((grad_content, grad_rel), (key_part, value_part))

    inner_state, block_parts = lax.scan(
        back_one_step,
        (back_start_state[0], back_start_state[1]),
        jnp.arange(extent // back_step_rows, dtype=jnp.int32),
    )
    key_all = block_parts[0].reshape(extent, D)
    value_all = block_parts[1].reshape(extent, D)
    grad_content, grad_rel, key_all, value_all = (
        inner_state[0],
        inner_state[1],
        key_all,
        value_all,
    )
    grad_keys, grad_values = (
        lax.psum_scatter(key_all, "tm", scatter_dimension=0, tiled=True),
        lax.psum_scatter(value_all, "tm", scatter_dimension=0, tiled=True),
    )
    half_size = D // 2
    rel_first = grad_rel[..., :half_size]
    rel_second = grad_rel[..., half_size:]
    sine_wide = sine_rows[:, None, :]
    cosine_wide = cosine_rows[:, None, :]
    grad_projected = jnp.concatenate(
        [
            rel_first * sine_wide - rel_second * cosine_wide,
            rel_first * cosine_wide + rel_second * sine_wide,
        ],
        axis=-1,
    ).astype(jnp.bfloat16)
    grad_pos_weight = jnp.einsum(
        "thc,the->che", grad_projected, position_heads, preferred_element_type=jnp.float32
    ).reshape(D, D)
    grad_q_position = jnp.einsum(
        "thc,che->the", grad_projected, pos_heads, preferred_element_type=jnp.float32
    )
    grad_content_bias = jnp.sum(grad_content, axis=0).reshape(D)
    grad_position_bias = jnp.sum(grad_q_position, axis=0).reshape(D)
    grad_query = (grad_content + grad_q_position).reshape(row_count, D).astype(jnp.bfloat16)
    grad_qkv = jnp.concatenate(
        [grad_query, grad_keys.astype(jnp.bfloat16), grad_values.astype(jnp.bfloat16)], axis=1
    )
    grad_qkv_weight = jnp.einsum(
        "tc,tf->cf", attn_norm_low, grad_qkv, preferred_element_type=jnp.float32
    )
    grad_attn_norm = jnp.einsum(
        "tf,cf->tc", grad_qkv, qkv_weight, preferred_element_type=jnp.float32
    )
    grad_from_attn, grad_ln_attn_gain, grad_ln_attn_bias = attn_pull(grad_attn_norm)
    grad_from_mlp, grad_ln_mlp_gain, grad_ln_mlp_bias = mlp_pull(grad_mlp_norm)
    grad_inputs = grad_rows + grad_from_attn + grad_from_mlp
    weight_grads = (
        grad_ln_attn_gain,
        grad_ln_attn_bias,
        grad_ln_mlp_gain,
        grad_ln_mlp_bias,
        grad_qkv_weight,
        grad_content_bias,
        grad_position_bias,
        grad_pos_weight,
        grad_out_weight,
        grad_up_weight,
        grad_up_bias,
        grad_gate_norm_gain,
        grad_gate_norm_bias,
        grad_conv_kernel,
        grad_conv_bias,
        grad_down_weight,
        grad_down_bias,
        grad_merge_weight,
        grad_merge_bias,
    )
    summed = lax.psum(
        (
            weight_grads[0],
            weight_grads[1],
            weight_grads[2],
            weight_grads[3],
            weight_grads[4],
            weight_grads[5],
            weight_grads[6],
            weight_grads[7],
            weight_grads[8],
            weight_grads[9],
            weight_grads[10],
            weight_grads[11],
            weight_grads[12],
            weight_grads[13],
            weight_grads[14],
            weight_grads[15],
            weight_grads[16],
            weight_grads[17],
            weight_grads[18],
        ),
        "tm",
    )
    shares = (
        lax.psum_scatter(
            summed[0].astype(jnp.bfloat16), "stream", scatter_dimension=0, tiled=True
        ).astype(jnp.float32),
        lax.psum_scatter(
            summed[1].astype(jnp.bfloat16), "stream", scatter_dimension=0, tiled=True
        ).astype(jnp.float32),
        lax.psum_scatter(
            summed[2].astype(jnp.bfloat16), "stream", scatter_dimension=0, tiled=True
        ).astype(jnp.float32),
        lax.psum_scatter(
            summed[3].astype(jnp.bfloat16), "stream", scatter_dimension=0, tiled=True
        ).astype(jnp.float32),
        lax.psum_scatter(
            summed[4].astype(jnp.bfloat16), "stream", scatter_dimension=0, tiled=True
        ).astype(jnp.float32),
        lax.psum_scatter(
            summed[5].astype(jnp.bfloat16), "stream", scatter_dimension=0, tiled=True
        ).astype(jnp.float32),
        lax.psum_scatter(
            summed[6].astype(jnp.bfloat16), "stream", scatter_dimension=0, tiled=True
        ).astype(jnp.float32),
        lax.psum_scatter(
            summed[7].astype(jnp.bfloat16), "stream", scatter_dimension=0, tiled=True
        ).astype(jnp.float32),
        lax.psum_scatter(
            summed[8].astype(jnp.bfloat16), "stream", scatter_dimension=0, tiled=True
        ).astype(jnp.float32),
        lax.psum_scatter(
            summed[9].astype(jnp.bfloat16), "stream", scatter_dimension=0, tiled=True
        ).astype(jnp.float32),
        lax.psum_scatter(
            summed[10].astype(jnp.bfloat16), "stream", scatter_dimension=0, tiled=True
        ).astype(jnp.float32),
        lax.psum_scatter(
            summed[11].astype(jnp.bfloat16), "stream", scatter_dimension=0, tiled=True
        ).astype(jnp.float32),
        lax.psum_scatter(
            summed[12].astype(jnp.bfloat16), "stream", scatter_dimension=0, tiled=True
        ).astype(jnp.float32),
        lax.psum_scatter(
            summed[13].astype(jnp.bfloat16), "stream", scatter_dimension=1, tiled=True
        ).astype(jnp.float32),
        lax.psum_scatter(
            summed[14].astype(jnp.bfloat16), "stream", scatter_dimension=0, tiled=True
        ).astype(jnp.float32),
        lax.psum_scatter(
            summed[15].astype(jnp.bfloat16), "stream", scatter_dimension=0, tiled=True
        ).astype(jnp.float32),
        lax.psum_scatter(
            summed[16].astype(jnp.bfloat16), "stream", scatter_dimension=0, tiled=True
        ).astype(jnp.float32),
        lax.psum_scatter(
            summed[17].astype(jnp.bfloat16), "stream", scatter_dimension=0, tiled=True
        ).astype(jnp.float32),
        lax.psum_scatter(
            summed[18].astype(jnp.bfloat16), "stream", scatter_dimension=0, tiled=True
        ).astype(jnp.float32),
    )
    return (out_rows, grad_inputs[None]) + tuple(shares)


LANES = 128
LOW = LANES // 2
BLOCK = 128
TALL = 256
WINDOW = 64
MARGIN = 16
BOUNDS = 16
MEGA = 1024 * 1024
F32 = jnp.float32
BF16 = jnp.bfloat16


def dot_nn(left, right):
    return jnp.dot(left, right, preferred_element_type=F32)


def dot_nt(left, right):
    return lax.dot_general(left, right, (((1,), (1,)), ((), ())), preferred_element_type=F32)


def dot_tn(left, right):
    return lax.dot_general(left, right, (((0,), (0,)), ((), ())), preferred_element_type=F32)


def rows_of(index, size, base=0):
    return pl.ds(pl.multiple_of(index * size, size) + base, size)


def line_of(ref):
    return ref[...].astype(F32).reshape(1, ref.shape[0])


def fold_rows(values):
    return jnp.sum(values.reshape(values.shape[0] // 8, 8, values.shape[1]), axis=0)


def one_row(values):
    return jnp.sum(values, axis=0, keepdims=True)


def turn(values):
    return pltpu.roll(values, LOW, 1)


def low_lanes(rows):
    return lax.broadcasted_iota(jnp.int32, (rows, LANES), 1) < LOW


def centre_rows(inputs):
    mean = jnp.mean(inputs, axis=-1, keepdims=True)
    centred = inputs - mean
    spread = jnp.mean(centred * centred, axis=-1, keepdims=True)
    return centred * lax.rsqrt(spread + EPS)


def gelu_parts(values):
    phi = 0.5 + 0.5 * lax.erf(values * math.sqrt(0.5))
    bell = jnp.exp(values * values * -0.5)
    return values * phi, phi + values * bell * (1.0 / math.sqrt(2.0 * math.pi))


class Part:
    def __init__(self, shape=None, pairs=None, refs=1, late=False):
        self.shape, self.pairs, self.refs, self.late = shape, pairs, refs, late

    def buffer(self, operand):
        return self.shape or operand.shape

    def copies(self, refs, buffer):
        return self.pairs(refs, buffer) if self.pairs else [(refs[0], buffer)]


def blocks_part(late=False):
    def pairs(refs, buffer):
        place = lax.axis_index("tm")
        return [
            (ref, buffer.at[rows_of(lax.bitwise_xor(jnp.int32(apart), place), BLOCK)])
            for apart, ref in enumerate(refs)
        ]

    return Part((HEADS * BLOCK, D), pairs, HEADS, late)


def rows_part(first, size, late=False):
    return Part((size, D), lambda refs, buffer: [(refs[0].at[pl.ds(first, size)], buffer)], late=late)


class Fetch:
    def __init__(self, pairs, buffer, sems, first):
        self.buffer, self.begun = buffer, False
        self.pending = [
            pltpu.make_async_copy(source, target, sems.at[first + index])
            for index, (source, target) in enumerate(pairs)
        ]

    def begin(self):
        if not self.begun:
            for copy in self.pending:
                copy.start()
        self.begun = True

    def __call__(self):
        self.begin()
        for copy in self.pending:
            copy.wait()
        self.pending = []
        return self.buffer


def begin(*fetches):
    for fetch in fetches:
        fetch.begin()


class Send:
    def __init__(self, buffer, target, sems):
        self.buffer, self.target, self.sems, self.copies = buffer, target, sems, []

    def go(self, *index):
        source, target = (self.buffer.at[index], self.target.at[index]) if index else (self.buffer, self.target)
        copy = pltpu.make_async_copy(source, target, self.sems[len(self.copies)])
        copy.start()
        self.copies.append(copy)

    def finish(self):
        if not self.copies:
            self.go()


SPACES = {"v": pltpu.VMEM, "s": pltpu.SMEM, "k": pl.ANY}


def kernel_call(body, out_shapes, plan, scratch=(), megas=58, bounds=False, aliases=None):
    def call(*operands):
        in_specs, buffers, at = [], [], 0
        for item in plan:
            if item == "f":
                in_specs.append(pl.BlockSpec(memory_space=pl.ANY))
                buffers.append(pltpu.VMEM(operands[at].shape, operands[at].dtype))
                at += 1
            elif isinstance(item, Part):
                in_specs += [pl.BlockSpec(memory_space=pl.ANY)] * item.refs
                buffers.append(pltpu.VMEM(item.buffer(operands[at]), operands[at].dtype))
                at += item.refs
            else:
                in_specs.append(pl.BlockSpec(memory_space=SPACES[item]))
                at += 1
        sent = [out for out in out_shapes if len(out) > 2]
        buffers += [pltpu.VMEM(out[3] if len(out) > 3 else out[0], out[1]) for out in sent]
        sem_count = 96
        extra = [pltpu.SMEM((BOUNDS,), jnp.int32)] if bounds else []

        def outer(*refs):
            inputs, rest = refs[: len(in_specs)], refs[len(in_specs) :]
            outputs, rest = rest[: len(out_shapes)], rest[len(out_shapes) :]
            held, rest = list(rest[: len(buffers)]), rest[len(buffers) :]
            sems, rest = rest[0], rest[1:]
            given, at, used = [], 0, 0
            for item in plan:
                if item == "f":
                    given.append(Fetch([(inputs[at], held[0])], held.pop(0), sems, used))
                    given[-1].begin()
                    used += 1
                    at += 1
                elif isinstance(item, Part):
                    buffer = held.pop(0)
                    pairs = item.copies(inputs[at : at + item.refs], buffer)
                    given.append(Fetch(pairs, buffer, sems, used))
                    if not item.late:
                        given[-1].begin()
                    used += len(pairs)
                    at += item.refs
                else:
                    given.append(inputs[at])
                    at += 1
            results = []
            for out, ref in zip(out_shapes, outputs):
                if len(out) > 2:
                    target = out[4](ref) if len(out) > 3 else ref
                    results.append(Send(held.pop(0), target, [sems.at[used + index] for index in range(4)]))
                    used += 4
                else:
                    results.append(ref)
            assert used <= sem_count
            given = [item() if kind == "f" else item for kind, item in zip(plan, given)]
            body(*given, *results, *rest)
            for item in given:
                if isinstance(item, Fetch):
                    item()
            sends = [item for item in results if isinstance(item, Send)]
            for item in sends:
                item.finish()
            for item in sends:
                for copy in item.copies:
                    copy.wait()

        return pl.pallas_call(
            outer,
            out_shape=[jax.ShapeDtypeStruct(out[0], out[1]) for out in out_shapes],
            in_specs=in_specs,
            out_specs=[pl.BlockSpec(memory_space=pl.ANY if len(out) > 2 else pltpu.VMEM) for out in out_shapes],
            scratch_shapes=buffers
            + [pltpu.SemaphoreType.DMA((sem_count,))]
            + [pltpu.VMEM(shape, kind) for shape, kind in scratch]
            + extra,
            input_output_aliases=aliases or {},
            compiler_params=pltpu.CompilerParams(vmem_limit_bytes=megas * MEGA),
            cost_estimate=pl.CostEstimate(flops=0, bytes_accessed=0, transcendentals=0),
        )(*operands)

    return call


def fill_bounds(lengths_ref, bounds_s, total):
    bounds_s[0] = jnp.int32(0)
    end = jnp.int32(0)
    for item in range(ITEMS):
        end = end + lengths_ref[0, item]
        bounds_s[item + 1] = end
    for item in range(ITEMS + 1, BOUNDS):
        bounds_s[item] = jnp.int32(total)


def head_lanes(values):
    odd = lax.rem(lax.axis_index("tm"), 2) == 1
    return jnp.where(low_lanes(values.shape[0]), jnp.where(odd, turn(values), values), 0.0)


def head_line(ref):
    values = line_of(ref)
    pair = lax.div(lax.axis_index("tm"), 2)
    picked = values[:, :LANES]
    for tile in range(1, D // LANES):
        picked = jnp.where(pair == tile, values[:, tile * LANES : (tile + 1) * LANES], picked)
    return head_lanes(picked)


def select_channels(up_ref, lines, taps_ref, up_out, table_out):
    place = lax.axis_index("tm")
    quarters = lax.axis_size("stream")
    share = HALF // (quarters * lax.axis_size("tm"))
    lane = lax.broadcasted_iota(jnp.int32, (1, 2 * LANES), 1)
    channel = jnp.where(lane < LANES + LOW, lane, lane - LOW)
    group = jnp.zeros_like(channel)
    for quarter in range(1, quarters):
        group = group + (channel >= quarter * share).astype(jnp.int32)
    source = group * (HALF // quarters) + share * place + channel - group * share
    chosen = (lax.broadcasted_iota(jnp.int32, (HALF, 2 * LANES), 0) == source).astype(F32).astype(BF16)
    gate = dot_nn(up_ref[:, :HALF], chosen)
    conv = dot_nn(up_ref[:, HALF:], chosen)
    up_out[:, :LANES] = gate[:, :LANES].astype(BF16)
    up_out[:, LANES : 2 * LANES] = jnp.where(low_lanes(D), gate[:, LANES:], conv[:, LANES:]).astype(BF16)
    up_out[:, 2 * LANES :] = conv[:, :LANES].astype(BF16)
    lines = dot_nn(lines.astype(BF16), chosen)
    taps = dot_nn(taps_ref[...], chosen)
    for part in range(2):
        lanes = slice(part * LANES, (part + 1) * LANES)
        table_out[part, :8] = lines[:, lanes]
        table_out[part, 8 : 8 + KERNEL] = taps[:, lanes]
        table_out[part, 8 + KERNEL :] = jnp.zeros((1, LANES), F32)


def angle_rows(coarse_ref, fine_ref, block, rows):
    half = D // 2
    base = coarse_ref[pl.ds(block, 1)]
    base_sine, base_cosine = base[:, :half], base[:, half:]
    sine, cosine = fine_ref[rows, :half], fine_ref[rows, half:]
    return base_sine * cosine + base_cosine * sine, base_cosine * cosine - base_sine * sine


def item_codes(bounds_s, index):
    code = jnp.zeros_like(index)
    for item in range(1, ITEMS + 1):
        code = code + (index >= bounds_s[item]).astype(jnp.int32)
    return jnp.where(code < ITEMS, code, ITEMS + index)


def attend_kernel(
    lengths_ref,
    x_ref,
    attn_gain_ref,
    attn_bias_ref,
    mlp_gain_ref,
    mlp_bias_ref,
    qkv_ref,
    pos_ref,
    content_ref,
    position_ref,
    coarse_ref,
    fine_ref,
    up_ref,
    up_bias_ref,
    gate_gain_ref,
    gate_bias_ref,
    conv_bias_ref,
    taps_ref,
    up_out,
    table_out,
    qkv_out,
    pos_out,
    n_attn_out,
    n_mlp_out,
    hat_out,
    q_position_out,
    query_out,
    key_out,
    value_out,
    prob_out,
    attn_out,
    stats_out,
    bounds_s,
):
    frames = n_attn_out.buffer.shape[0]
    half = D // 2
    fill_bounds(lengths_ref, bounds_s, frames)
    attn_gain, attn_bias = line_of(attn_gain_ref), line_of(attn_bias_ref)
    mlp_gain, mlp_bias = line_of(mlp_gain_ref), line_of(mlp_bias_ref)
    content, position = head_line(content_ref), head_line(position_ref)
    x_ref, qkv_ref, pos_ref = x_ref(), qkv_ref(), pos_ref()
    begin(up_ref)
    for part in range(3):
        lanes = slice(part * LANES, (part + 1) * LANES)
        qkv_out.buffer[:, lanes] = head_lanes(qkv_ref[:, lanes].astype(F32)).astype(BF16)
    pos_out.buffer[...] = head_lanes(pos_ref[...].astype(F32)).astype(BF16)
    qkv_out.go()
    pos_out.go()

    @pl.loop(0, frames // TALL, unroll=4)
    def _(block):
        rows = rows_of(block, TALL)
        for part in range(TALL // 32):
            at = pl.ds(pl.multiple_of(block * TALL + part * 32, 32), 32)
            hat = centre_rows(x_ref[at].astype(F32))
            hat_out.buffer[at] = hat.astype(BF16)
            n_attn_out.buffer[at] = (hat * attn_gain + attn_bias).astype(BF16)
            n_mlp_out.buffer[at] = (hat * mlp_gain + mlp_bias).astype(BF16)
        parts = dot_nn(n_attn_out.buffer[rows], qkv_out.buffer[...])
        query = parts[:, :LANES]
        query_out.buffer[rows, :LANES] = ((query + content).astype(BF16).astype(F32) * 0.125).astype(BF16)
        q_position = (query + position).astype(BF16)
        q_position_out.buffer[rows] = q_position
        key_out.buffer[rows, :LANES] = parts[:, LANES : 2 * LANES].astype(BF16)
        value_out.buffer[rows] = parts[:, 2 * LANES :].astype(BF16)
        projected = dot_nt(q_position, pos_out.buffer[...])
        for part in range(TALL // 32):
            at = pl.ds(pl.multiple_of(block * TALL + part * 32, 32), 32)
            inner = part * 32 % BLOCK
            sine, cosine = angle_rows(
                coarse_ref, fine_ref, block * (TALL // BLOCK) + part * 32 // BLOCK, slice(inner, inner + 32)
            )
            first = projected[part * 32 : part * 32 + 32, :half]
            second = projected[part * 32 : part * 32 + 32, half:]
            query_out.buffer[at, LANES : LANES + half] = ((first * sine + second * cosine) * 0.125).astype(BF16)
            query_out.buffer[at, LANES + half :] = ((second * sine - first * cosine) * 0.125).astype(BF16)
            key_out.buffer[at, LANES : LANES + half] = cosine.astype(BF16)
            key_out.buffer[at, LANES + half :] = sine.astype(BF16)

    for out in (n_attn_out, n_mlp_out, hat_out, q_position_out, query_out, key_out, value_out):
        out.go()
    up_ref = up_ref()
    up_bias = line_of(up_bias_ref)
    lines = [up_bias[:, :HALF], up_bias[:, HALF:]]
    lines += [line_of(ref) for ref in (gate_gain_ref, gate_bias_ref, conv_bias_ref)]
    lines = jnp.concatenate(lines + [jnp.zeros((3, HALF), F32)], axis=0)
    select_channels(up_ref, lines, taps_ref, up_out.buffer, table_out.buffer)
    up_out.go()
    table_out.go()
    up_bias = up_bias[:, HALF:]
    lane = lax.broadcasted_iota(jnp.int32, (16, LANES), 1)

    @pl.loop(0, frames // TALL, unroll=2)
    def _(block):
        values = dot_nn(n_mlp_out.buffer[rows_of(block, TALL)], up_ref[:, HALF:])
        for part in range(TALL // 16):
            pre = values[part * 16 : part * 16 + 16] + up_bias
            hidden = pre * (0.5 + 0.5 * lax.erf(pre * math.sqrt(0.5)))
            mean = jnp.mean(hidden, axis=-1, keepdims=True)
            centred = hidden - mean
            rate = lax.rsqrt(jnp.mean(centred * centred, axis=-1, keepdims=True) + EPS)
            at = pl.ds(pl.multiple_of(block * TALL + part * 16, 16), 16)
            stats_out.buffer[at] = jnp.where(lane == 0, mean, rate)

    stats_out.go()
    key_code = item_codes(bounds_s, lax.broadcasted_iota(jnp.int32, (1, frames), 1))

    low = low_lanes(32)
    for block in range(frames // TALL):
        rows = pl.ds(block * TALL, TALL)
        raw = dot_nt(query_out.buffer[rows], key_out.buffer[...])
        shares = []
        for part in range(TALL // 32):
            start = block * TALL + part * 32
            index = start + lax.broadcasted_iota(jnp.int32, (32, 1), 0)
            scaled = jnp.where(
                item_codes(bounds_s, index) == key_code, raw[part * 32 : part * 32 + 32], MASKED
            )
            weight = jnp.exp(scaled - jnp.max(scaled, axis=1, keepdims=True))
            prob_out.buffer[pl.ds(start, 32)] = weight.astype(BF16)
            shares.append(1.0 / jnp.sum(weight, axis=1, keepdims=True))
        prob_out.go(rows)
        attn = dot_nn(prob_out.buffer[rows], value_out.buffer[...])
        for part in range(TALL // 32):
            share = shares[part]
            attn_out.buffer[pl.ds(block * TALL + part * 32, 32)] = jnp.where(
                low, attn[part * 32 : part * 32 + 32] * share, share
            )


def fill_margins(wide_s, frames):
    edge = jnp.zeros((MARGIN, LANES), F32)
    wide_s[:MARGIN] = edge
    wide_s[MARGIN + frames : 2 * MARGIN + frames] = edge
    base = frames + 3 * MARGIN
    after = base + frames // 2
    low = low_lanes(MARGIN)
    wide_s[base - MARGIN : base] = jnp.where(low, 0.0, turn(wide_s[after - MARGIN : after]))
    wide_s[after : after + MARGIN] = jnp.where(low, turn(wide_s[base : base + MARGIN]), 0.0)


def item_span(bounds_s, frame):
    begin, end = bounds_s[0], bounds_s[BOUNDS - 1]
    for item in range(1, ITEMS + 1):
        edge = bounds_s[item]
        begin = jnp.where(frame >= edge, edge, begin)
    for item in range(ITEMS, 0, -1):
        edge = bounds_s[item]
        end = jnp.where(frame < edge, edge, end)
    return begin, end


def is_whole(bounds_s, start):
    begin, end = item_span(bounds_s, start)
    reach = KERNEL // 2
    low = (begin == 0) | (begin <= start - reach)
    high = (end == bounds_s[BOUNDS - 1]) | (end >= start + WINDOW + reach)
    return low & high & (end >= start + WINDOW)


def tap_limits(bounds_s, start):
    frame = start + lax.broadcasted_iota(jnp.int32, (WINDOW, LANES), 0)
    begin, end = item_span(bounds_s, frame)
    return begin - frame, end - frame


def grouped(values):
    return values.reshape(WINDOW // 8, 8, LANES)


def triple_places(step, frames):
    half = frames // 2
    return (
        pl.multiple_of(step * WINDOW, 2 * MARGIN),
        pl.multiple_of(step * WINDOW + half, 2 * MARGIN),
        pl.multiple_of(step * WINDOW + frames + 2 * MARGIN, 2 * MARGIN),
    )


def over_windows(bounds_s, frames, body):
    half = frames // 2

    @pl.loop(0, half // WINDOW)
    def _(step):
        start = step * WINDOW
        whole = is_whole(bounds_s, start) & is_whole(bounds_s, start + half)

        @pl.when(whole)
        def _():
            body(step, None)

        @pl.when(jnp.logical_not(whole))
        def _():
            first, second = tap_limits(bounds_s, start), tap_limits(bounds_s, start + half)
            low = low_lanes(WINDOW)
            rest = [jnp.where(low, one, other) for one, other in zip(first, second)]
            body(step, (first, second, rest))


def tap_view(window_ref, tap, limits):
    view = window_ref[tap + 1 : tap + 1 + WINDOW]
    if limits is not None:
        shift = tap - KERNEL // 2
        view = jnp.where((limits[0] <= shift) & (limits[1] > shift), view, 0.0)
    return grouped(view)


def mlp_first_kernel(
    lengths_ref,
    n_ref,
    up_ref,
    table_ref,
    stats_ref,
    cot_ref,
    merge_ref,
    down_ref,
    attn_ref,
    mixed_out,
    gate_pre_out,
    grad_out,
    rate_out,
    hat_out,
    early_out,
    vectors_out,
    lines_out,
    hat_s,
    slope_s,
    gate_s,
    hidden_s,
    gate_slope_s,
    conv_s,
    grad_s,
    out_s,
    back_s,
    branch_s,
    mix_s,
    taps_s,
    turn_s,
    tap_sum_s,
    columns_s,
    forward_s,
    backward_s,
    bounds_s,
):
    frames = mix_s.shape[0]
    half = frames // 2
    blocks = frames // BLOCK
    quarters, early_rows, _ = early_out.buffer.shape
    share = early_rows // 8
    channels = quarters * share
    fill_bounds(lengths_ref, bounds_s, frames)
    table_ref, up_ref = table_ref(), up_ref()
    for part in range(2):
        for tap in range(KERNEL):
            line = jnp.broadcast_to(table_ref[part, 8 + tap : 9 + tap], (8, LANES))
            taps_s[part, tap] = line
            turn_s[part, KERNEL - 1 - tap] = line
    tap_sum_s[...] = jnp.zeros(tap_sum_s.shape, F32)
    main, rest = table_ref[0, :8], table_ref[1, :8]
    mixed_bias = jnp.where(low_lanes(1), rest[0:1], rest[1:2])
    low = low_lanes(64)
    gate_pre_ref = gate_pre_out.buffer
    n_ref = n_ref()
    stats_ref = stats_ref()
    begin(cot_ref, merge_ref, down_ref, attn_ref)

    def stat_rows(rows):
        stats = stats_ref[rows]
        return stats[:, 0:1], stats[:, 1:2]

    def chunk(start, base=0):
        return pl.ds(pl.multiple_of(start, 64) + base, 64)

    def conv_part(hidden, mean, rate, lines, rows, to_rows):
        hat = (hidden - mean) * rate
        hat_s[rows] = hat
        hat_out.buffer[rows] = hat.astype(BF16)
        conv_s[to_rows] = (hat * lines[2:3] + lines[3:4]).astype(BF16).astype(F32)

    @pl.loop(0, half // TALL, unroll=2)
    def _(block):
        pre = [dot_nn(n_ref[rows_of(block, TALL, base)], up_ref[...]) for base in (0, half)]
        for part in range(TALL // 64):
            inner = slice(part * 64, part * 64 + 64)
            start = block * TALL + part * 64
            mixed = []
            for values, base in zip(pre, (0, half)):
                rows = chunk(start, base)
                gate, gate_slope = gelu_parts(values[inner, :LANES] + main[0:1])
                hidden_s[rows] = gate
                gate_slope_s[rows] = gate_slope
                hidden, slope = gelu_parts(values[inner, 2 * LANES :] + main[1:2])
                mean, rate = stat_rows(rows)
                slope_s[rows] = slope * rate
                conv_part(hidden, mean, rate, main, rows, chunk(start, base + MARGIN))
                mixed.append((*gelu_parts(values[inner, LANES : 2 * LANES] + mixed_bias), mean, rate))
            (low_hidden, low_slope, low_mean, low_rate), (high_hidden, high_slope, high_mean, high_rate) = mixed
            rows = chunk(start, frames)
            hidden_s[rows] = jnp.where(low, low_hidden, turn(high_hidden))
            gate_slope_s[rows] = jnp.where(low, low_slope, turn(high_slope))
            rate = jnp.where(low, low_rate, high_rate)
            slope_s[rows] = jnp.where(low, turn(low_slope), high_slope) * rate
            conv_part(
                jnp.where(low, turn(low_hidden), high_hidden),
                jnp.where(low, low_mean, high_mean),
                rate,
                rest,
                rows,
                chunk(start, frames + 3 * MARGIN),
            )

    hat_out.go()
    fill_margins(conv_s, frames)
    tall = WINDOW + 2 * MARGIN
    outs = (0, half, frames)

    def convolve(step, limits):
        for index, base in enumerate(triple_places(step, frames)):
            forward_s[index] = conv_s[pl.ds(base, tall)]
        for index in range(3):
            own = None if limits is None else limits[index]
            total = jnp.zeros((WINDOW // 8, 8, LANES), F32)
            for tap in range(KERNEL):
                total = total + tap_view(forward_s.at[index], tap, own) * taps_s[index // 2, tap][None]
            lines = rest if index == 2 else main
            out_s[rows_of(step, WINDOW, outs[index])] = total.reshape(WINDOW, LANES) + lines[4:5]

    over_windows(bounds_s, frames, convolve)
    cot_ref = cot_ref()
    merge_ref = merge_ref()
    down_ref = down_ref()
    attn_ref = attn_ref()
    down_ref[channels:] = jnp.zeros((2 * LANES - channels, D), BF16)
    zero = jnp.zeros((8, LANES), F32)

    def branch_part(grad_gated, rows, to_rows, sums):
        up_sum, conv_sum = sums
        gate, conv = hidden_s[rows], out_s[rows]
        gate_pre = (grad_gated * conv * gate_slope_s[rows]).astype(BF16)
        gate_pre_ref[rows] = gate_pre
        grad_conv = (grad_gated * gate).astype(BF16).astype(F32)
        grad_s[to_rows] = grad_conv
        gate_pre = gate_pre.astype(F32)
        return gate * conv, gate_pre, (up_sum + fold_rows(gate_pre), conv_sum + fold_rows(grad_conv))

    def branch_step(block, sums):
        main_sums, rest_sums = sums
        grads = []
        for base in (0, half):
            rows = rows_of(block, TALL, base)
            branch = dot_nt(cot_ref[rows], merge_ref[...]).astype(BF16)
            branch_s[rows] = branch
            grads.append(dot_nt(branch, down_ref[...]))
        for part in range(TALL // 64):
            inner = slice(part * 64, part * 64 + 64)
            start = block * TALL + part * 64
            for values, base in zip(grads, (0, half)):
                rows = chunk(start, base)
                gated, gate_pre, main_sums = branch_part(
                    values[inner, :LANES], rows, chunk(start, base + MARGIN), main_sums
                )
                mix_s[rows, :LANES] = gated.astype(BF16)
                gate_s[rows, :LANES] = gate_pre.astype(BF16)
            grad = jnp.where(low, grads[0][inner, LANES:], turn(grads[1][inner, LANES:]))
            gated, gate_pre, rest_sums = branch_part(
                grad, chunk(start, frames), chunk(start, frames + 3 * MARGIN), rest_sums
            )
            low_rows, high_rows = chunk(start), chunk(start, half)
            gate_s[low_rows, LANES:] = gate_pre.astype(BF16)
            gate_s[high_rows, LANES:] = turn(gate_pre).astype(BF16)
            mix_s[low_rows, LANES:] = jnp.where(low, gated, turn(attn_ref[low_rows])).astype(BF16)
            mix_s[high_rows, LANES:] = jnp.where(low, turn(gated), turn(attn_ref[high_rows])).astype(BF16)
        return main_sums, rest_sums

    (main_up, main_conv), (rest_up, rest_conv) = lax.fori_loop(
        0, half // TALL, branch_step, ((zero, zero), (zero, zero)), unroll=2
    )
    gate_pre_out.go()
    fill_margins(grad_s, frames)
    ones = jnp.ones((16, frames), BF16)
    lines_out[0:1] = dot_nn(ones, branch_s[...])[0:1]
    lines_out[1:2] = dot_nn(ones, cot_ref[...])[0:1]
    lines_out[2:8] = jnp.zeros((6, D), F32)
    grad_down = dot_tn(mix_s[...], branch_s[...])
    grad_gate = dot_tn(gate_s[...], n_ref[...])
    for quarter in range(quarters):
        for tile in range(4):
            early_out.buffer[quarter, tile * share : (tile + 1) * share] = grad_down[
                quarter * share : (quarter + 1) * share, tile * LANES : (tile + 1) * LANES
            ].astype(BF16)
        early_out.buffer[quarter, 4 * share :] = grad_gate[
            :channels, quarter * LANES : (quarter + 1) * LANES
        ].astype(BF16)
    early_out.go()
    for block in range(blocks):
        mixed_out.buffer[block, :BLOCK] = mix_s[block * BLOCK : (block + 1) * BLOCK]
    mixed_out.go(slice(None), pl.ds(0, BLOCK))

    def differentiate(step, limits):
        for index, base in enumerate(triple_places(step, frames)):
            forward_s[index] = conv_s[pl.ds(base, tall)]
            backward_s[index] = grad_s[pl.ds(base, tall)]
        for index in range(3):
            own = None if limits is None else limits[index]
            total = jnp.zeros((WINDOW // 8, 8, LANES), F32)
            centre = grouped(backward_s[index, MARGIN : MARGIN + WINDOW])
            for tap in range(KERNEL):
                total = total + tap_view(backward_s.at[index], tap, own) * turn_s[index // 2, tap][None]
                tap_sum_s[index // 2, tap] += jnp.sum(tap_view(forward_s.at[index], tap, own) * centre, axis=0)
            back_s[rows_of(step, WINDOW, outs[index])] = total.reshape(WINDOW, LANES)

    over_windows(bounds_s, frames, differentiate)
    lane = lax.broadcasted_iota(jnp.int32, (64, LANES), 1)

    def norm_part(rows, lines, sums):
        gain_sum, bias_sum = sums
        back, hat, slope = back_s[rows], hat_s[rows], slope_s[rows]
        grad = back * lines[2:3]
        grad_out.buffer[rows] = (grad * slope).astype(BF16)
        rate_out.buffer[rows] = slope.astype(BF16)
        along = back * hat
        return grad, along * lines[2:3], (gain_sum + fold_rows(along), bias_sum + fold_rows(back))

    def norm_step(block, sums):
        main_sums, rest_sums = sums
        for part in range(TALL // 64):
            start = block * TALL + part * 64
            pairs = []
            for base in (0, half):
                plain, along, main_sums = norm_part(chunk(start, base), main, main_sums)
                pairs.append([plain, along])
            plain, along, rest_sums = norm_part(chunk(start, frames), rest, rest_sums)
            for item, values in enumerate((plain, along)):
                pairs[0][item] = pairs[0][item] + jnp.where(low, values, 0.0)
                pairs[1][item] = pairs[1][item] + jnp.where(low, 0.0, values)
            for (plain, along), base in zip(pairs, (0, half)):
                columns_s[chunk(start, base)] = jnp.where(
                    lane == 0,
                    jnp.sum(plain, axis=-1, keepdims=True),
                    jnp.where(lane == 1, jnp.sum(along, axis=-1, keepdims=True), 0.0),
                )
        return main_sums, rest_sums

    (main_gain, main_bias), (rest_gain, rest_bias) = lax.fori_loop(
        0, half // TALL, norm_step, ((zero, zero), (zero, zero)), unroll=2
    )
    grad_out.go()
    rate_out.go()
    totals = jnp.concatenate(
        [jnp.transpose(columns_s[block * BLOCK : (block + 1) * BLOCK])[:2] for block in range(blocks)], axis=0
    )
    high = totals.astype(BF16)
    low_part = (totals - high.astype(F32)).astype(BF16)
    for block in range(blocks):
        mixed_out.buffer[block, BLOCK:, :LANES] = high
        mixed_out.buffer[block, BLOCK:, LANES:] = low_part
    mixed_out.go(slice(None), pl.ds(BLOCK, 2 * blocks))

    def vectors(part, lines):
        taps = jnp.sum(tap_sum_s[part], axis=1)[:KERNEL]
        stacked = jnp.concatenate([taps] + [one_row(line) for line in lines], axis=0)
        if part:
            stacked = stacked + turn(stacked)
        return jnp.transpose(
            jnp.concatenate([stacked, jnp.zeros((LANES - stacked.shape[0], LANES), F32)], axis=0)
        )

    vectors_out[:LANES] = vectors(0, (main_conv, main_gain, main_bias, main_up))
    vectors_out[LANES:] = vectors(1, (rest_conv, rest_gain, rest_bias, rest_up))[: channels - LANES]


def attend_back_kernel(
    cot_ref,
    merge_ref,
    head_ref,
    attn_ref,
    value_ref,
    prob_ref,
    key_ref,
    coarse_ref,
    fine_ref,
    pos_ref,
    query_ref,
    n_ref,
    q_position_ref,
    qkv_ref,
    hat_ref,
    gain_ref,
    early_ref,
    branch_out,
    total_out,
    pack_0,
    pack_1,
    pack_2,
    pack_3,
    lines_out,
    grad_s,
    raw_s,
    projected_s,
    parts_s,
    grads_s,
):
    place = lax.axis_index("tm")
    frames = raw_s.shape[0]
    blocks = frames // BLOCK
    half = D // 2
    zero = jnp.zeros((8, LANES), F32)
    cot_ref, merge_ref, head_ref, attn_ref = cot_ref(), merge_ref(), head_ref(), attn_ref()
    head_ref[HEAD:] = jnp.zeros((LANES - HEAD, D), BF16)
    begin(value_ref, prob_ref, key_ref, pos_ref)

    @pl.loop(0, frames // TALL, unroll=4)
    def _(block):
        rows = rows_of(block, TALL)
        branch = dot_nt(cot_ref[rows], merge_ref[...]).astype(BF16)
        branch_out.buffer[rows] = branch
        grad_s[rows] = (dot_nt(branch, head_ref[...]) * attn_ref[rows, HEAD : HEAD + 1]).astype(BF16)

    branch_out.go()
    value_ref, prob_ref = value_ref(), prob_ref()
    key_ref, pos_ref = key_ref(), pos_ref()
    begin(query_ref, n_ref, q_position_ref, qkv_ref, hat_ref, early_ref)

    def score_step(block, sums):
        content_sum, position_sum = sums
        rows = rows_of(block, TALL)
        grad = grad_s[rows]
        score = dot_nt(grad, value_ref[...])
        for part in range(TALL // 32):
            at = pl.ds(pl.multiple_of(block * TALL + part * 32, 32), 32)
            inner = slice(part * 32, part * 32 + 32)
            delta = jnp.sum(grad[inner].astype(F32) * attn_ref[at], axis=1, keepdims=True)
            raw_s[at] = (prob_ref[at].astype(F32) * (score[inner] - delta)).astype(BF16)
        query = dot_nn(raw_s[rows], key_ref[...]) * 0.125
        for part in range(TALL // 32):
            at = pl.ds(pl.multiple_of(block * TALL + part * 32, 32), 32)
            inner = part * 32 % BLOCK
            sine, cosine = angle_rows(
                coarse_ref, fine_ref, block * (TALL // BLOCK) + part * 32 // BLOCK, slice(inner, inner + 32)
            )
            inner = slice(part * 32, part * 32 + 32)
            first, second = query[inner, LANES : LANES + half], query[inner, LANES + half :]
            projected_s[at, :half] = (first * sine - second * cosine).astype(BF16)
            projected_s[at, half:] = (first * cosine + second * sine).astype(BF16)
        position = dot_nn(projected_s[rows], pos_ref[...])
        content = query[:, :LANES]
        parts_s[rows, :LANES] = (content + position).astype(BF16)
        return content_sum + fold_rows(content), position_sum + fold_rows(position)

    content_sum, position_sum = lax.fori_loop(0, frames // TALL, score_step, (zero, zero), unroll=4)
    query_ref, n_ref, q_position_ref = query_ref(), n_ref(), q_position_ref()
    qkv_ref, hat_ref = qkv_ref(), hat_ref()
    grad_key = dot_tn(query_ref[...], raw_s[...])
    grad_value = dot_tn(grad_s[...], prob_ref[...])
    for block in range(blocks):
        at = slice(block * BLOCK, (block + 1) * BLOCK)
        parts_s[at, LANES : 2 * LANES] = jnp.transpose(grad_key[:, at]).astype(BF16)
        parts_s[at, 2 * LANES :] = jnp.transpose(grad_value[:, at]).astype(BF16)
    grads_s[:HEAD] = dot_tn(parts_s[:, :LANES], n_ref[...])[:HEAD]
    grads_s[HEAD : 2 * HEAD] = dot_nn(grad_key.astype(BF16), n_ref[...])[:HEAD]
    grads_s[2 * HEAD : 3 * HEAD] = dot_nn(grad_value.astype(BF16), n_ref[...])[:HEAD]
    grads_s[3 * HEAD :] = dot_tn(q_position_ref[...], projected_s[...])[:HEAD]
    stream = lax.axis_index("stream")
    early_ref = early_ref()
    for apart, pack_out in enumerate((pack_0, pack_1, pack_2, pack_3)):
        quarter = lax.bitwise_xor(stream, jnp.int32(apart))
        lanes = pl.ds(pl.multiple_of(quarter * LANES, LANES), LANES)
        pack_out.buffer[: 4 * HEAD] = grads_s[:, lanes].astype(BF16)
        pack_out.buffer[4 * HEAD :] = early_ref[quarter]
        pack_out.go()
    gain = line_of(gain_ref)
    wide_zero = jnp.zeros((8, D), F32)

    def norm_step(block, sums):
        gain_sum, bias_sum = sums
        grad = dot_nt(parts_s[rows_of(block, TALL)], qkv_ref[...])
        for part in range(TALL // 32):
            at = pl.ds(pl.multiple_of(block * TALL + part * 32, 32), 32)
            own = grad[part * 32 : part * 32 + 32]
            total_out.buffer[at] = (own * gain).astype(BF16)
            gain_sum = gain_sum + fold_rows(own * hat_ref[at].astype(F32))
            bias_sum = bias_sum + fold_rows(own)
        return gain_sum, bias_sum

    gain_sum, bias_sum = lax.fori_loop(0, frames // TALL, norm_step, (wide_zero, wide_zero), unroll=4)
    lane = lax.broadcasted_iota(jnp.int32, (1, LANES), 1)

    def own_lanes(sums):
        line = one_row(sums)
        line = line + turn(line)
        tiles = [
            jnp.where(lax.div(tile * LANES + lane, HEAD) == place, line, 0.0) for tile in range(D // LANES)
        ]
        return jnp.concatenate(tiles, axis=1)

    lines_out[...] = jnp.concatenate(
        [
            one_row(gain_sum),
            one_row(bias_sum),
            own_lanes(content_sum),
            own_lanes(position_sum),
            jnp.zeros((4, D), F32),
        ],
        axis=0,
    )


def mlp_second_kernel(
    mixed_ref,
    gate_pre_ref,
    grad_ref,
    rate_ref,
    hat_ref,
    up_ref,
    norm_hat_ref,
    gain_ref,
    other_ref,
    n_ref,
    vectors_ref,
    first_lines_ref,
    head_lines_ref,
    total_out,
    pack_0,
    pack_1,
    pack_2,
    pack_3,
    pre_s,
    columns_s,
    grad_up_s,
    lines_s,
    up_columns_s,
):
    packs = (pack_0, pack_1, pack_2, pack_3)
    stream = lax.axis_index("stream")
    place = lax.axis_index("tm")
    frames = pre_s.shape[0]
    half = frames // 2
    blocks = frames // BLOCK
    quarters = len(packs)
    channels = vectors_ref.shape[0]
    share = channels // quarters
    totals = jnp.zeros((2 * blocks, LANES), F32)
    mixed_ref = mixed_ref()
    for source in range(mixed_ref.shape[0]):
        both = mixed_ref[source].astype(F32)
        totals = totals + (both[:, :LANES] + both[:, LANES:])
    totals = totals * (1.0 / HALF)
    columns = jnp.transpose(jnp.concatenate([totals, jnp.zeros((LANES - 2 * blocks, LANES), F32)], axis=0))
    lane = lax.broadcasted_iota(jnp.int32, (BLOCK, LANES), 1)
    for block in range(blocks):
        columns_s[block * BLOCK : (block + 1) * BLOCK] = jnp.where(
            lane == 0, columns[:, 2 * block : 2 * block + 1], columns[:, 2 * block + 1 : 2 * block + 2]
        )
    gate_pre_ref, grad_ref, rate_ref, hat_ref = gate_pre_ref(), grad_ref(), rate_ref(), hat_ref()
    begin(n_ref, up_ref, norm_hat_ref, other_ref)
    low = low_lanes(64)
    gain = line_of(gain_ref)

    def chunk(start, base=0):
        return pl.ds(pl.multiple_of(start, 64) + base, 64)

    def pre_part(rows, table, up_sum):
        plain, along = table
        hat, rate = hat_ref[rows].astype(F32), rate_ref[rows].astype(F32)
        pre = (grad_ref[rows].astype(F32) - rate * (plain + hat * along)).astype(BF16).astype(F32)
        return pre, up_sum + fold_rows(pre)

    def pre_step(block, sums):
        main_up, rest_up = sums
        for part in range(TALL // 64):
            start = block * TALL + part * 64
            tables = []
            for base in (0, half):
                rows = chunk(start, base)
                values = columns_s[rows]
                table = [values[:, item : item + 1] for item in range(2)]
                tables.append(table)
                pre, main_up = pre_part(rows, table, main_up)
                pre_s[rows, :LANES] = gate_pre_ref[rows]
                pre_s[rows, 2 * LANES :] = pre.astype(BF16)
            rows = chunk(start, frames)
            table = [jnp.where(low, one, other) for one, other in zip(*tables)]
            pre, rest_up = pre_part(rows, table, rest_up)
            gate_pre = gate_pre_ref[rows].astype(F32)
            pre_s[chunk(start), LANES : 2 * LANES] = jnp.where(low, gate_pre, turn(pre)).astype(BF16)
            pre_s[chunk(start, half), LANES : 2 * LANES] = jnp.where(low, turn(gate_pre), pre).astype(BF16)
        return main_up, rest_up

    zero = jnp.zeros((8, LANES), F32)
    main_up, rest_up = lax.fori_loop(0, half // TALL, pre_step, (zero, zero), unroll=2)
    n_ref, up_ref, norm_hat_ref, other_ref = n_ref(), up_ref(), norm_hat_ref(), other_ref()
    grad_up_s[...] = dot_tn(pre_s[:, LANES:], n_ref[...])
    wide_zero = jnp.zeros((8, D), F32)

    def norm_step(block, sums):
        gain_sum, bias_sum = sums
        rows = rows_of(block, BLOCK)
        grad = dot_nt(pre_s[rows], up_ref[...])
        total_out.buffer[block] = (grad * gain + other_ref[rows].astype(F32)).astype(BF16)
        return gain_sum + fold_rows(grad * norm_hat_ref[rows].astype(F32)), bias_sum + fold_rows(grad)

    gain_sum, bias_sum = lax.fori_loop(0, blocks, norm_step, (wide_zero, wide_zero), unroll=4)
    total_out.go()
    rest_line = one_row(rest_up)
    up_columns_s[:LANES] = jnp.transpose(jnp.broadcast_to(one_row(main_up), (LANES, LANES)))
    up_columns_s[LANES:] = jnp.transpose(jnp.broadcast_to(rest_line + turn(rest_line), (LANES, LANES)))[:LOW]
    first_device = (place == 0).astype(F32)
    lines_s[...] = jnp.concatenate(
        [
            head_lines_ref[0:2],
            one_row(gain_sum),
            one_row(bias_sum),
            head_lines_ref[2:4],
            first_lines_ref[0:2] * first_device,
            jnp.zeros((8, D), F32),
        ],
        axis=0,
    )
    gate_at = KERNEL + 3
    lane = lax.broadcasted_iota(jnp.int32, (share, LANES), 1)
    for apart, pack_out in enumerate(packs):
        quarter = lax.bitwise_xor(stream, jnp.int32(apart))
        lanes = pl.ds(pl.multiple_of(quarter * LANES, LANES), LANES)
        pack_out[:LANES] = grad_up_s[LANES:, lanes].astype(BF16)
        pack_out[LANES:channels] = grad_up_s[LOW:LANES, lanes].astype(BF16)
        table = vectors_ref[pl.ds(pl.multiple_of(quarter * share, 8), share)]
        for other in range(2):
            at = pl.ds(pl.multiple_of((2 * lax.rem(quarter, 2) + other) * share, 8), share)
            column = jnp.where(
                quarter < quarters // 2, vectors_ref[at][:, gate_at : gate_at + 1], up_columns_s[at][:, 0:1]
            )
            table = jnp.where(lane == gate_at + other, column, table)
        pack_out[channels : channels + share] = table.astype(BF16)
        pack_out[channels + share :] = lines_s[:, lanes].astype(BF16)


def output_kernel(
    x_ref, mixed_ref, head_ref, down_ref, down_bias_ref, merge_ref, merge_bias_ref, out_ref, joined_out
):
    sources = mixed_ref.shape[0]
    rows = x_ref.shape[0]
    channels = HALF // sources
    share = channels // 4
    attn_parts = []
    branch_attn = jnp.zeros((rows, D), F32)
    branch_mlp = jnp.zeros((rows, D), F32)
    for source in range(sources):
        attn = turn(mixed_ref[source, :rows, LANES:].astype(F32))[:, :HEAD].astype(BF16)
        attn_parts.append(attn)
        branch_attn = branch_attn + dot_nn(attn, head_ref[source * HEAD : (source + 1) * HEAD])
        down = jnp.concatenate(
            [down_ref[(part * sources + source) * share : (part * sources + source + 1) * share] for part in range(4)],
            axis=0,
        )
        branch_mlp = branch_mlp + dot_nn(mixed_ref[source, :rows, :channels], down)
    joined = jnp.concatenate(
        [branch_attn.astype(BF16), (branch_mlp + line_of(down_bias_ref)).astype(BF16)], axis=1
    )
    result = x_ref[...].astype(F32) + dot_nn(joined, merge_ref[...]) + line_of(merge_bias_ref)
    out_ref.buffer[...] = result.astype(BF16)
    out_ref.go()
    joined_out = joined_out.buffer
    turned = jnp.transpose(joined.astype(F32))
    heads = jnp.transpose(jnp.concatenate(attn_parts, axis=1).astype(F32))
    merge_share = turned.shape[0] // (4 * sources)
    head_share = heads.shape[0] // (4 * sources)
    used = 4 * (merge_share + head_share)
    for target in range(sources):
        for part in range(4):
            at = (part * sources + target) * merge_share
            joined_out[target, part * merge_share : (part + 1) * merge_share] = turned[
                at : at + merge_share
            ].astype(BF16)
            at = (part * sources + target) * head_share
            to = 4 * merge_share + part * head_share
            joined_out[target, to : to + head_share] = heads[at : at + head_share].astype(BF16)
        joined_out[target, used:] = jnp.zeros((joined_out.shape[1] - used, rows), BF16)


def merge_kernel(joined_ref, branch_ref, cot_ref, pack_0, pack_1, pack_2, pack_3, merge_s, head_s):
    stream = lax.axis_index("stream")
    cot_ref = cot_ref()
    sources, _, rows = joined_ref.shape
    merge_rows = 2 * D // sources
    head_rows = D // sources
    grad_merge = jnp.zeros((merge_rows, D), F32)
    grad_head = jnp.zeros((head_rows, D), F32)
    for source in range(sources):
        at = slice(source * rows, (source + 1) * rows)
        joined = joined_ref[source]
        grad_merge = grad_merge + dot_nn(joined[:merge_rows], cot_ref[at])
        grad_head = grad_head + dot_nn(joined[merge_rows : merge_rows + head_rows], branch_ref[at])
    merge_s[...] = grad_merge
    head_s[...] = grad_head
    for apart, pack_out in enumerate((pack_0, pack_1, pack_2, pack_3)):
        pack_out = pack_out.buffer
        quarter = lax.bitwise_xor(stream, jnp.int32(apart))
        for grad_s, base in ((merge_s, 0), (head_s, merge_rows)):
            share = grad_s.shape[0] // 4
            at = pl.ds(pl.multiple_of(quarter * share, share), share)
            for tile in range(4):
                to = base + tile * share
                pack_out[to : to + share] = grad_s[at, tile * LANES : (tile + 1) * LANES].astype(BF16)


def frames_kernel(x_ref, cot_ref, total_ref, out_ref):
    for part in range(x_ref.shape[0] // 32):
        rows = slice(part * 32, part * 32 + 32)
        inputs = x_ref[rows].astype(F32)
        mean = jnp.mean(inputs, axis=-1, keepdims=True)
        centred = inputs - mean
        rate = lax.rsqrt(jnp.mean(centred * centred, axis=-1, keepdims=True) + EPS)
        hat = centred * rate
        grad = total_ref[0, rows].astype(F32)
        for source in range(1, total_ref.shape[0]):
            grad = grad + total_ref[source, rows].astype(F32)
        plain = jnp.mean(grad, axis=-1, keepdims=True)
        along = jnp.mean(grad * hat, axis=-1, keepdims=True)
        out_ref[rows] = cot_ref[rows].astype(F32) + rate * (grad - plain - hat * along)


def add_kernel(*refs):
    out_ref = refs[-1]
    first = 0
    for at in range(0, len(refs) - 1, 4):
        total = refs[at][...].astype(F32)
        for ref in refs[at + 1 : at + 4]:
            total = total + ref[...].astype(F32)
        out_ref[first : first + total.shape[0]] = total.astype(BF16)
        first += total.shape[0]


def gather_parts(near_ref, far_ref, all_s):
    place = lax.axis_index("tm")
    for apart in range(all_s.shape[0]):
        part_ref = far_ref if apart % 2 else near_ref
        all_s[lax.bitwise_xor(jnp.int32(apart), place)] = part_ref[apart // 2]


def lines_from(all_s, base, size):
    return jnp.concatenate([all_s[source, base : base + size] for source in range(all_s.shape[0])], axis=0).astype(F32)


def early_kernel(near_ref, far_ref, qkv_out, pos_out, down_out, up_out, all_s):
    gather_parts(near_ref, far_ref, all_s)
    sources = all_s.shape[0]
    share = HALF // (4 * sources)
    for kind in range(4):
        lines = jnp.transpose(lines_from(all_s, kind * HEAD, HEAD))
        if kind < 3:
            qkv_out[:, kind * D : (kind + 1) * D] = lines
        else:
            pos_out[...] = lines
    base = 4 * HEAD
    for source in range(sources):
        for tile in range(4):
            down_out[source * share : (source + 1) * share, tile * LANES : (tile + 1) * LANES] = all_s[
                source, base + tile * share : base + (tile + 1) * share
            ].astype(F32)
    wide = sources * share
    for group in range(4):
        up_out.buffer[:, group * wide : (group + 1) * wide] = jnp.transpose(
            lines_from(all_s, base + 4 * share + group * share, share)
        )


def late_kernel(*refs):
    _, near_ref, far_ref = refs[:3]
    (
        attn_gain_out,
        attn_bias_out,
        mlp_gain_out,
        mlp_bias_out,
        content_out,
        position_out,
        outw_out,
        up_out,
        up_bias_out,
        gain_out,
        bias_out,
        taps_out,
        conv_bias_out,
        down_bias_out,
        merge_out,
        merge_bias_out,
        all_s,
    ) = refs[3:]
    gather_parts(near_ref, far_ref, all_s)
    sources = all_s.shape[0]
    channels = HALF // sources
    share = channels // 4
    base = 0
    for group in range(4):
        at = group * sources * share
        up_out.buffer[:, at : at + sources * share] = jnp.transpose(lines_from(all_s, base + group * share, share))
    up_out.go()
    table = jnp.transpose(lines_from(all_s, base + channels, share))
    taps_out[...] = table[:KERNEL]
    conv_bias_out[...] = table[KERNEL]
    gain_out[...] = table[KERNEL + 1]
    bias_out[...] = table[KERNEL + 2]
    wide = sources * share
    up_bias_out[:wide] = table[KERNEL + 3]
    up_bias_out[wide:] = table[KERNEL + 4]
    base = base + channels + share
    lines = all_s[0, base : base + 16].astype(F32)
    for source in range(1, sources):
        lines = lines + all_s[source, base : base + 16].astype(F32)
    outs = (attn_gain_out, attn_bias_out, mlp_gain_out, mlp_bias_out, content_out, position_out, down_bias_out, merge_bias_out)
    for line, out in enumerate(outs):
        out[...] = lines[line]
    base = base + 16
    merge_share = 2 * D // (4 * sources)
    head_share = D // (4 * sources)
    for source in range(sources):
        for tile in range(4):
            lanes = slice(tile * LANES, (tile + 1) * LANES)
            at = base + tile * merge_share
            merge_out[source * merge_share : (source + 1) * merge_share, lanes] = all_s[
                source, at : at + merge_share
            ].astype(F32)
            at = base + 4 * merge_share + tile * head_share
            outw_out[source * head_share : (source + 1) * head_share, lanes] = all_s[
                source, at : at + head_share
            ].astype(F32)


def moved(block, axis, bits):
    count = lax.axis_size(axis)
    return lax.ppermute(block, axis, [(index, index ^ bits) for index in range(count)])


def over_streams(packs):
    return [packs[0]] + [moved(packs[bits], "stream", bits) for bits in range(1, lax.axis_size("stream"))]


def near_blocks(block):
    return [block] + [moved(block, "tm", bits) for bits in range(2, lax.axis_size("tm"), 2)]


def far_blocks(near):
    far = [moved(part, "tm", 1) for part in near]
    return [part for pair in zip(near, far) for part in pair]


def far_stack(near):
    stack = jnp.stack(near)
    return stack, moved(stack, "tm", 1)


def head_device(
    frames,
    lengths,
    cotangent,
    ln_attn_gain,
    ln_attn_bias,
    ln_mlp_gain,
    ln_mlp_bias,
    qkv_weight,
    content_bias,
    position_bias,
    pos_weight,
    out_weight,
    up_weight,
    up_bias,
    gate_norm_gain,
    gate_norm_bias,
    conv_kernel,
    conv_bias,
    down_weight,
    down_bias,
    merge_weight,
    merge_bias,
):
    count = lax.axis_size("tm")
    quarters = lax.axis_size("stream")
    own = frames.shape[1]
    total = own * count
    folded = total + total // 2
    padded = folded + 4 * MARGIN
    share = HALF // (quarters * count)
    channels = HALF // count
    quarter = D // quarters
    own_frames = frames[0]
    own_cotangent = cotangent[0]

    whole, late = Part(), Part(late=True)
    near = near_blocks(own_frames)
    cot_near = near_blocks(own_cotangent)
    blocks = far_blocks(near)
    frequency = jnp.exp(jnp.arange(D // 2, dtype=F32) * (-2.0 * math.log(10000.0) / D))
    coarse = jnp.arange(0, total, BLOCK, dtype=F32)[:, None] * frequency[None]
    fine = jnp.arange(BLOCK, dtype=F32)[:, None] * frequency[None]
    coarse_table = jnp.concatenate([jnp.sin(coarse), jnp.cos(coarse)], axis=1)
    fine_table = jnp.concatenate([jnp.sin(fine), jnp.cos(fine)], axis=1)

    def own_lanes(count):
        def pairs(refs, buffer):
            base = lax.div(lax.axis_index("tm"), 2) * LANES
            return [
                (
                    refs[0].at[:, pl.ds(pl.multiple_of(base + part * D, LANES), LANES)],
                    buffer.at[:, pl.ds(part * LANES, LANES)],
                )
                for part in range(count)
            ]

        return Part((D, count * LANES), pairs)

    up_own, table, qkv_own, pos_own, n_attn, n_mlp, hat, q_position, query, key, value, prob, attn, stats = kernel_call(
        attend_kernel,
        [
            ((D, 3 * LANES), BF16, 1),
            ((2, 8 + KERNEL + 1, LANES), F32, 1),
            ((D, 3 * LANES), BF16, 1),
            ((D, LANES), BF16, 1),
            ((total, D), BF16, 1),
            ((total, D), BF16, 1),
            ((total, D), BF16, 1),
            ((total, LANES), BF16, 1),
            ((total, LANES + D), BF16, 1),
            ((total, LANES + D), BF16, 1),
            ((total, LANES), BF16, 1),
            ((total, total), BF16, 1),
            ((total, LANES), F32, 1),
            ((total, LANES), F32, 1),
        ],
        [
            "s",
            blocks_part(),
            *"vvvv",
            own_lanes(3),
            own_lanes(1),
            *"vvvv",
            late,
            *"vvvvv",
        ],
        bounds=True,
    )(
        lengths,
        *blocks,
        ln_attn_gain,
        ln_attn_bias,
        ln_mlp_gain,
        ln_mlp_bias,
        qkv_weight,
        pos_weight,
        content_bias,
        position_bias,
        coarse_table,
        fine_table,
        up_weight,
        up_bias,
        gate_norm_gain,
        gate_norm_bias,
        conv_bias,
        conv_kernel,
    )
    n_mlp, cot_near = lax.optimization_barrier((n_mlp, cot_near))
    cot = far_blocks(cot_near)

    def own_down(refs, buffer):
        place = lax.axis_index("tm")
        stride = HALF // quarters
        return [
            (
                refs[0].at[pl.ds(pl.multiple_of(part * stride + share * place, 16), share)],
                buffer.at[pl.ds(part * share, share)],
            )
            for part in range(quarters)
        ]

    mixed, gate_pre, grad_y, slope, gate_hat, early_pack, vectors, first_lines = kernel_call(
        mlp_first_kernel,
        [
            ((count, own + 16, 2 * LANES), BF16, 1),
            ((folded, LANES), BF16, 1),
            ((folded, LANES), BF16, 1),
            ((folded, LANES), BF16, 1),
            ((folded, LANES), BF16, 1),
            ((quarters, 8 * share, LANES), BF16, 1),
            ((channels, LANES), F32),
            ((8, D), F32),
        ],
        [
            "s",
            whole,
            whole,
            whole,
            whole,
            blocks_part(late=True),
            rows_part(D, D, late=True),
            Part((2 * LANES, D), own_down, late=True),
            Part(late=True),
        ],
        [
            ((folded, LANES), F32),
            ((folded, LANES), F32),
            ((total, 2 * LANES), BF16),
            ((folded, LANES), F32),
            ((folded, LANES), F32),
            ((padded, LANES), F32),
            ((padded, LANES), F32),
            ((folded, LANES), F32),
            ((folded, LANES), F32),
            ((total, D), BF16),
            ((total, 2 * LANES), BF16),
            ((2, 32, 8, LANES), F32),
            ((2, 32, 8, LANES), F32),
            ((2, 32, 8, LANES), F32),
            ((total, LANES), F32),
            ((3, WINDOW + 2 * MARGIN, LANES), F32),
            ((3, WINDOW + 2 * MARGIN, LANES), F32),
        ],
        bounds=True,
    )(lengths, n_mlp, up_own, table, stats, *cot, merge_weight, down_weight, attn)
    mixed_own = lax.all_to_all(mixed, "tm", 0, 0, tiled=True)

    def own_head(refs, buffer):
        at = pl.ds(pl.multiple_of(lax.axis_index("tm") * HEAD, HEAD), HEAD)
        return [(refs[0].at[at], buffer.at[pl.ds(0, HEAD)])]

    branch, from_attn, *head_packs, head_lines = kernel_call(
        attend_back_kernel,
        [
            ((total, D), BF16, 1),
            ((total, D), BF16, 1),
            *([((4 * HEAD + 8 * share, LANES), BF16, 1)] * quarters),
            ((8, D), F32),
        ],
        [
            blocks_part(),
            rows_part(0, D),
            Part((LANES, D), own_head),
            whole,
            late,
            late,
            late,
            "v",
            "v",
            late,
            Part((total, LANES), lambda refs, buffer: [(refs[0].at[:, pl.ds(0, LANES)], buffer)], late=True),
            late,
            late,
            late,
            late,
            "v",
            late,
        ],
        [
            ((total, LANES), BF16),
            ((total, total), BF16),
            ((total, D), BF16),
            ((total, 3 * LANES), BF16),
            ((4 * HEAD, D), F32),
        ],
    )(
        *cot,
        merge_weight,
        out_weight,
        attn,
        value,
        prob,
        key,
        coarse_table,
        fine_table,
        pos_own,
        query,
        n_attn,
        q_position,
        qkv_own,
        hat,
        ln_attn_gain,
        early_pack,
    )
    head_parts = over_streams(head_packs)
    mixed_own, _ = lax.optimization_barrier((mixed_own, head_lines))
    out_rows, joined = kernel_call(
        output_kernel,
        [((own, D), BF16, 1), ((count, 256, own), BF16, 1)],
        ["f", "f", "f", "f", "v", "f", "v"],
    )(own_frames, mixed_own, out_weight, down_weight, down_bias, merge_weight, merge_bias)
    joined_all = lax.all_to_all(joined, "tm", 0, 0, tiled=True)
    gate_pre, _ = lax.optimization_barrier((gate_pre, joined))
    up_rows = 5 * share + 16
    from_both, *up_packs = kernel_call(
        mlp_second_kernel,
        [((count, own, D), BF16, 1)] + [((up_rows, LANES), BF16)] * quarters,
        [
            Part(
                (count, 2 * total // BLOCK, 2 * LANES),
                lambda refs, buffer: [(refs[0].at[:, pl.ds(own, 2 * total // BLOCK)], buffer)],
            ),
            *([whole] * 4),
            late,
            late,
            "v",
            late,
            late,
            *"vvv",
        ],
        [
            ((total, 3 * LANES), BF16),
            ((total, LANES), F32),
            ((2 * LANES, D), F32),
            ((16, D), F32),
            ((channels, LANES), F32),
        ],
    )(
        mixed_own,
        gate_pre,
        grad_y,
        slope,
        gate_hat,
        up_own,
        hat,
        ln_mlp_gain,
        from_attn,
        n_mlp,
        vectors,
        first_lines,
        head_lines,
    )
    up_parts = over_streams(up_packs)
    from_both, head_parts = lax.optimization_barrier((from_both, head_parts))
    from_all = lax.all_to_all(from_both, "tm", 0, 0, tiled=True)
    joined_all, up_parts[1] = lax.optimization_barrier((joined_all, up_parts[1]))
    merge_rows = 3 * D // count
    merge_packs = kernel_call(
        merge_kernel,
        [((merge_rows, LANES), BF16, 1)] * quarters,
        ["f", "f", blocks_part()],
        [((2 * D // count, D), F32), ((D // count, D), F32)],
    )(joined_all, branch, *cot)
    merge_parts = over_streams(merge_packs)
    head_parts, up_parts, _ = lax.optimization_barrier((head_parts, up_parts, merge_packs[0]))
    (early_part,) = kernel_call(add_kernel, [((4 * HEAD + 8 * share, LANES), BF16)], quarters * "v", megas=24)(
        *head_parts
    )
    early_near = near_blocks(early_part)
    (grad_frames,) = kernel_call(frames_kernel, [((own, D), F32)], "vvv", megas=24)(
        own_frames, own_cotangent, from_all
    )
    early_near, merge_parts, grad_frames = lax.optimization_barrier((early_near, merge_parts, grad_frames))
    late_rows = up_rows + merge_rows
    (late_part,) = kernel_call(add_kernel, [((late_rows, LANES), BF16)], 2 * quarters * "v", megas=24)(
        *up_parts, *merge_parts
    )
    late_near = near_blocks(late_part)
    early_all = far_stack(early_near)
    grad_qkv, grad_pos, grad_down, half_up = kernel_call(
        early_kernel,
        [
            ((quarter, 3 * D), F32),
            ((quarter, D), F32),
            ((HALF // quarters, D), F32),
            ((quarter, 2 * HALF), F32, 1, (quarter, HALF), lambda ref: ref.at[:, pl.ds(0, HALF)]),
        ],
        "vv",
        [((count, 4 * HEAD + 8 * share, LANES), BF16)],
        megas=24,
    )(*early_all)
    late_near, grad_frames, grad_pos = lax.optimization_barrier((late_near, grad_frames, grad_pos))
    late_parts = far_stack(late_near)
    late = kernel_call(
        late_kernel,
        [((quarter,), F32)] * 6
        + [
            ((quarter, D), F32),
            ((quarter, 2 * HALF), F32, 1, (quarter, HALF), lambda ref: ref.at[:, pl.ds(HALF, HALF)]),
            ((2 * HALF // quarters,), F32),
            ((HALF // quarters,), F32),
            ((HALF // quarters,), F32),
            ((KERNEL, HALF // quarters), F32),
            ((HALF // quarters,), F32),
            ((quarter,), F32),
            ((2 * D // quarters, D), F32),
            ((quarter,), F32),
        ],
        "kvv",
        [((count,) + late_part.shape, BF16)],
        megas=24,
        aliases={0: 7},
    )(half_up, *late_parts)
    return (
        out_rows[None],
        grad_frames[None],
        *late[:4],
        grad_qkv,
        *late[4:6],
        grad_pos,
        *late[6:13],
        grad_down,
        *late[13:],
    )


def per_device(*operands):
    fits = (
        lax.axis_size("tm") == HEADS
        and lax.axis_size("stream") * LANES == D
        and operands[0].shape[1] == BLOCK
    )
    return head_device(*operands) if fits else frame_device(*operands)


def solution(mesh):
    return jax.shard_map(
        per_device,
        mesh=mesh,
        in_specs=(
            P("stream", "tm", None),
            P("stream", None),
            P("stream", "tm", None),
            P(),
            P(),
            P(),
            P(),
            P(),
            P(),
            P(),
            P(),
            P(),
            P(),
            P(),
            P(),
            P(),
            P(),
            P(),
            P(),
            P(),
            P(),
            P(),
        ),
        out_specs=(
            P("stream", "tm", None),
            P("stream", "tm", None),
            P("stream"),
            P("stream"),
            P("stream"),
            P("stream"),
            P("stream", None),
            P("stream"),
            P("stream"),
            P("stream", None),
            P("stream", None),
            P("stream", None),
            P("stream"),
            P("stream"),
            P("stream"),
            P(None, "stream"),
            P("stream"),
            P("stream", None),
            P("stream"),
            P("stream", None),
            P("stream"),
        ),
        check_vma=False,
    )
```

```python
import math

import jax
import jax.numpy as jnp
from jax import lax
from jax.experimental import pallas as pl
from jax.experimental.pallas import tpu as pltpu
from jax.sharding import PartitionSpec as P

D = 512
HEADS = 8
HEAD = 64
KERNEL = 31
ITEMS = 5
HALF = 1536


EPS = 1e-05
MASKED = -1e30


def extended(block, sides, width):
    for axis, dim in sides:
        count = lax.axis_size(axis)
        forward = [(i, i + 1) for i in range(count - 1)]
        backward = [(target, source) for source, target in forward]
        low = lax.ppermute(
            lax.slice_in_dim(block, block.shape[dim] - width, None, axis=dim), axis, forward
        )
        high = lax.ppermute(lax.slice_in_dim(block, 0, width, axis=dim), axis, backward)
        block = jnp.concatenate([low, block, high], axis=dim)
    return block


def norm_rows(inputs, scale_row, shift_row):
    row_mean = jnp.mean(inputs, axis=-1, keepdims=True)
    centred = inputs - row_mean
    spread = jnp.mean(centred * centred, axis=-1, keepdims=True)
    return centred * lax.rsqrt(spread + EPS) * scale_row + shift_row


def gelu_exact(inputs):
    return jax.nn.gelu(inputs, approximate=False)


def frame_info(lengths, offset, extent):
    item_ends = jnp.cumsum(lengths)
    first_table = jnp.concatenate([item_ends - lengths, item_ends[-1:]])
    frame_index = offset + jnp.arange(extent, dtype=jnp.int32)
    item_of = jnp.sum((frame_index[:, None] >= item_ends[None, :]).astype(jnp.int32), axis=1)
    labels = jnp.arange(ITEMS + 1, dtype=jnp.int32)
    first_frame = jnp.sum(
        jnp.where(item_of[:, None] == labels[None, :], first_table[None, :], 0), axis=1
    )
    return (frame_index, item_of, frame_index - first_frame)


def angles(place_in):
    frequency = jnp.exp(jnp.arange(D // 2, dtype=jnp.float32) * (-2.0 * math.log(10000.0) / D))
    phase_angle = place_in.astype(jnp.float32)[:, None] * frequency[None, :]
    return (jnp.sin(phase_angle), jnp.cos(phase_angle))


def rel_query(projected, sine_rows, cosine_rows):
    half_size = projected.shape[-1] // 2
    first_half = projected[..., :half_size]
    second_half = projected[..., half_size:]
    sine_wide = sine_rows[:, None, :]
    cosine_wide = cosine_rows[:, None, :]
    return jnp.concatenate(
        [
            first_half * sine_wide + second_half * cosine_wide,
            second_half * sine_wide - first_half * cosine_wide,
        ],
        axis=-1,
    )


def step_size(extent):
    return math.gcd(extent, 512)


def score_block(q_content, q_rel, query_item, query_frame, key_block, key_start, lengths):
    extent = key_block.shape[0]
    key_frame, key_item, key_place = frame_info(lengths, key_start, extent)
    sine_rows, cosine_rows = angles(key_place)
    k_rel = jnp.concatenate([cosine_rows, sine_rows], axis=1).astype(jnp.bfloat16)
    raw_scores = jnp.einsum(
        "qhe,khe->hqk",
        q_content,
        key_block.reshape(extent, HEADS, HEAD),
        preferred_element_type=jnp.float32,
    )
    raw_scores = raw_scores + jnp.einsum(
        "qhc,kc->hqk", q_rel, k_rel, preferred_element_type=jnp.float32
    )
    allowed = (query_item[:, None] == key_item[None, :]) & (
        (query_item[:, None] < ITEMS) | (query_frame[:, None] == key_frame[None, :])
    )
    return (raw_scores, allowed, k_rel)


def block_grads(
    q_content,
    q_rel,
    query_item,
    query_frame,
    grad_out,
    log_total,
    delta_rows,
    key_block,
    value_block,
    key_start,
    lengths,
):
    extent = key_block.shape[0]
    raw_scores, allowed, k_rel = score_block(
        q_content, q_rel, query_item, query_frame, key_block, key_start, lengths
    )
    prob_rows = jnp.where(allowed[None], jnp.exp(raw_scores * 0.125 - log_total[:, :, None]), 0.0)
    grad_prob = jnp.einsum(
        "qhe,khe->hqk",
        grad_out,
        value_block.reshape(extent, HEADS, HEAD),
        preferred_element_type=jnp.float32,
    )
    grad_raw = (prob_rows * (grad_prob - delta_rows[:, :, None]) * 0.125).astype(jnp.bfloat16)
    return (prob_rows.astype(jnp.bfloat16), grad_raw, k_rel)


def frame_device(
    frames,
    lengths,
    cotangent,
    ln_attn_gain,
    ln_attn_bias,
    ln_mlp_gain,
    ln_mlp_bias,
    qkv_weight,
    content_bias,
    position_bias,
    pos_weight,
    out_weight,
    up_weight,
    up_bias,
    gate_norm_gain,
    gate_norm_bias,
    conv_kernel,
    conv_bias,
    down_weight,
    down_bias,
    merge_weight,
    merge_bias,
):
    row_count = frames.shape[1]
    cycle_size = lax.axis_size("tm")
    offset = lax.axis_index("tm") * row_count
    stream_lengths = lengths[0]
    inputs = frames[0].astype(jnp.float32)
    frame_index, item_of, place_in = frame_info(stream_lengths, offset, row_count)
    sine_rows, cosine_rows = angles(place_in)
    attn_norm, attn_pull = jax.vjp(
        norm_rows, inputs, ln_attn_gain.astype(jnp.float32), ln_attn_bias.astype(jnp.float32)
    )
    mlp_norm, mlp_pull = jax.vjp(
        norm_rows, inputs, ln_mlp_gain.astype(jnp.float32), ln_mlp_bias.astype(jnp.float32)
    )
    attn_norm_low = attn_norm.astype(jnp.bfloat16)
    mlp_norm_low = mlp_norm.astype(jnp.bfloat16)
    qkv_rows = jnp.dot(attn_norm_low, qkv_weight, preferred_element_type=jnp.float32)
    query_rows = qkv_rows[:, :D]
    key_rows = qkv_rows[:, D : 2 * D].astype(jnp.bfloat16)
    value_rows = qkv_rows[:, 2 * D :].astype(jnp.bfloat16)
    q_content = (query_rows + content_bias.astype(jnp.float32)).astype(jnp.bfloat16)
    q_position = (query_rows + position_bias.astype(jnp.float32)).astype(jnp.bfloat16)
    content_heads = q_content.reshape(row_count, HEADS, HEAD)
    position_heads = q_position.reshape(row_count, HEADS, HEAD)
    pos_heads = pos_weight.reshape(D, HEADS, HEAD)
    projected = jnp.einsum(
        "the,che->thc", position_heads, pos_heads, preferred_element_type=jnp.float32
    )
    q_rel = rel_query(projected, sine_rows, cosine_rows).astype(jnp.bfloat16)
    start_state = (
        jnp.full((HEADS, row_count), MASKED, jnp.float32),
        jnp.zeros((HEADS, row_count), jnp.float32),
        jnp.zeros((HEADS, row_count, HEAD), jnp.float32),
    )
    fold_state = start_state
    key_piece = lax.all_gather(key_rows, "tm", axis=0, tiled=True)
    value_piece = lax.all_gather(value_rows, "tm", axis=0, tiled=True)
    extent = key_piece.shape[0]
    step_rows = step_size(extent)

    def forward_one_step(inner_state, step_index):
        row_top, row_total, row_acc = inner_state
        key_block = lax.dynamic_slice_in_dim(key_piece, step_index * step_rows, step_rows, 0)
        value_block = lax.dynamic_slice_in_dim(value_piece, step_index * step_rows, step_rows, 0)
        raw_scores, allowed, k_rel = score_block(
            content_heads,
            q_rel,
            item_of,
            frame_index,
            key_block,
            step_index * step_rows,
            stream_lengths,
        )
        scaled = jnp.where(allowed[None], raw_scores * 0.125, MASKED)
        new_top = jnp.maximum(row_top, jnp.max(scaled, axis=2))
        weight = jnp.where(allowed[None], jnp.exp(scaled - new_top[:, :, None]), 0.0)
        factor = jnp.exp(row_top - new_top)
        row_total = row_total * factor + jnp.sum(weight, axis=2)
        row_acc = row_acc * factor[:, :, None] + jnp.einsum(
            "hqk,khe->hqe",
            weight.astype(jnp.bfloat16),
            value_block.reshape(step_rows, HEADS, HEAD),
            preferred_element_type=jnp.float32,
        )
        return ((new_top, row_total, row_acc), None)

    fold_state, unused = lax.scan(
        forward_one_step, fold_state, jnp.arange(extent // step_rows, dtype=jnp.int32)
    )
    row_top, row_total, row_acc = fold_state
    attn_heads = row_acc / row_total[:, :, None]
    log_total = row_top + jnp.log(row_total)
    attn_low = jnp.transpose(attn_heads, (1, 0, 2)).reshape(row_count, D).astype(jnp.bfloat16)
    branch_attn = jnp.dot(attn_low, out_weight, preferred_element_type=jnp.float32).astype(
        jnp.bfloat16
    )
    hidden_pre = jnp.dot(
        mlp_norm_low, up_weight, preferred_element_type=jnp.float32
    ) + up_bias.astype(jnp.float32)
    hidden, gelu_pull = jax.vjp(gelu_exact, hidden_pre)
    gate_half = hidden[:, :HALF]
    conv_norm, conv_pull = jax.vjp(
        norm_rows,
        hidden[:, HALF:],
        gate_norm_gain.astype(jnp.float32),
        gate_norm_bias.astype(jnp.float32),
    )
    conv_in = conv_norm.astype(jnp.bfloat16)
    half_width = KERNEL // 2
    conv_wide = extended(conv_in, (("tm", 0),), half_width)
    wide_frame, wide_item, wide_place = frame_info(
        stream_lengths, offset - half_width, row_count + 2 * half_width
    )
    kernel_rows = conv_kernel.astype(jnp.float32)
    conv_out = conv_bias.astype(jnp.float32) + jnp.zeros_like(gate_half)
    for tap_index in range(KERNEL):
        same_item = (wide_item[tap_index : tap_index + row_count] == item_of)[:, None]
        conv_out = (
            conv_out
            + jnp.where(
                same_item, conv_wide[tap_index : tap_index + row_count].astype(jnp.float32), 0.0
            )
            * kernel_rows[tap_index]
        )
    gated_low = (gate_half * conv_out).astype(jnp.bfloat16)
    branch_mlp = (
        jnp.dot(gated_low, down_weight, preferred_element_type=jnp.float32)
        + down_bias.astype(jnp.float32)
    ).astype(jnp.bfloat16)
    joined = jnp.concatenate([branch_attn, branch_mlp], axis=1)
    result = (
        inputs
        + jnp.dot(joined, merge_weight, preferred_element_type=jnp.float32)
        + merge_bias.astype(jnp.float32)
    )
    out_rows = result.astype(jnp.bfloat16)[None]
    grad_low = cotangent[0]
    grad_rows = grad_low.astype(jnp.float32)
    grad_merge_bias = jnp.sum(grad_rows, axis=0)
    grad_merge_weight = jnp.einsum(
        "tc,td->cd", joined, grad_low, preferred_element_type=jnp.float32
    )
    grad_joined = jnp.einsum(
        "td,cd->tc", grad_low, merge_weight, preferred_element_type=jnp.float32
    )
    grad_attn_branch = grad_joined[:, :D].astype(jnp.bfloat16)
    grad_mlp_branch = grad_joined[:, D:].astype(jnp.bfloat16)
    grad_down_weight = jnp.einsum(
        "tc,td->cd", gated_low, grad_mlp_branch, preferred_element_type=jnp.float32
    )
    grad_down_bias = jnp.sum(grad_mlp_branch.astype(jnp.float32), axis=0)
    grad_gated = jnp.einsum(
        "td,cd->tc", grad_mlp_branch, down_weight, preferred_element_type=jnp.float32
    )
    grad_gate_half = grad_gated * conv_out
    grad_conv_out = (grad_gated * gate_half).astype(jnp.bfloat16)
    grad_conv_rows = grad_conv_out.astype(jnp.float32)
    grad_conv_bias = jnp.sum(grad_conv_rows, axis=0)
    grad_wide = extended(grad_conv_out, (("tm", 0),), half_width)
    kernel_list = []
    grad_conv_in = jnp.zeros_like(grad_conv_rows)
    for tap_index in range(KERNEL):
        same_item = (wide_item[tap_index : tap_index + row_count] == item_of)[:, None]
        kernel_list.append(
            jnp.sum(
                jnp.where(
                    same_item, conv_wide[tap_index : tap_index + row_count].astype(jnp.float32), 0.0
                )
                * grad_conv_rows,
                axis=0,
            )
        )
        back_start = 2 * half_width - tap_index
        back_item = (wide_item[back_start : back_start + row_count] == item_of)[:, None]
        grad_conv_in = (
            grad_conv_in
            + jnp.where(
                back_item, grad_wide[back_start : back_start + row_count].astype(jnp.float32), 0.0
            )
            * kernel_rows[tap_index]
        )
    grad_conv_kernel = jnp.stack(kernel_list)
    grad_second, grad_gate_norm_gain, grad_gate_norm_bias = conv_pull(grad_conv_in)
    (grad_pre_rows,) = gelu_pull(jnp.concatenate([grad_gate_half, grad_second], axis=1))
    grad_pre = grad_pre_rows.astype(jnp.bfloat16)
    grad_up_bias = jnp.sum(grad_pre.astype(jnp.float32), axis=0)
    grad_up_weight = jnp.einsum(
        "tc,tf->cf", mlp_norm_low, grad_pre, preferred_element_type=jnp.float32
    )
    grad_mlp_norm = jnp.einsum("tf,cf->tc", grad_pre, up_weight, preferred_element_type=jnp.float32)
    grad_out_weight = jnp.einsum(
        "tc,td->cd", attn_low, grad_attn_branch, preferred_element_type=jnp.float32
    )
    grad_attn_low = jnp.einsum(
        "td,cd->tc", grad_attn_branch, out_weight, preferred_element_type=jnp.float32
    ).astype(jnp.bfloat16)
    grad_out_heads = grad_attn_low.reshape(row_count, HEADS, HEAD)
    delta_rows = jnp.sum(
        jnp.transpose(grad_out_heads.astype(jnp.float32), (1, 0, 2)) * attn_heads, axis=2
    )
    total_frames = row_count * cycle_size
    back_start_state = (
        jnp.zeros((row_count, HEADS, HEAD), jnp.float32),
        jnp.zeros((row_count, HEADS, D), jnp.float32),
        jnp.zeros((total_frames, D), jnp.float32),
        jnp.zeros((total_frames, D), jnp.float32),
    )
    back_key_piece = lax.all_gather(key_rows, "tm", axis=0, tiled=True)
    back_value_piece = lax.all_gather(value_rows, "tm", axis=0, tiled=True)
    extent = back_key_piece.shape[0]
    back_step_rows = step_size(extent)

    def back_one_step(inner_state, step_index):
        grad_content, grad_rel = inner_state
        key_block = lax.dynamic_slice_in_dim(
            back_key_piece, step_index * back_step_rows, back_step_rows, 0
        )
        value_block = lax.dynamic_slice_in_dim(
            back_value_piece, step_index * back_step_rows, back_step_rows, 0
        )
        prob_low, grad_raw, k_rel = block_grads(
            content_heads,
            q_rel,
            item_of,
            frame_index,
            grad_out_heads,
            log_total,
            delta_rows,
            key_block,
            value_block,
            step_index * back_step_rows,
            stream_lengths,
        )
        grad_content = grad_content + jnp.einsum(
            "hqk,khe->qhe",
            grad_raw,
            key_block.reshape(back_step_rows, HEADS, HEAD),
            preferred_element_type=jnp.float32,
        )
        grad_rel = grad_rel + jnp.einsum(
            "hqk,kc->qhc", grad_raw, k_rel, preferred_element_type=jnp.float32
        )
        key_part = jnp.einsum(
            "hqk,qhe->khe", grad_raw, content_heads, preferred_element_type=jnp.float32
        ).reshape(back_step_rows, D)
        value_part = jnp.einsum(
            "hqk,qhe->khe", prob_low, grad_out_heads, preferred_element_type=jnp.float32
        ).reshape(back_step_rows, D)
        return ((grad_content, grad_rel), (key_part, value_part))

    inner_state, block_parts = lax.scan(
        back_one_step,
        (back_start_state[0], back_start_state[1]),
        jnp.arange(extent // back_step_rows, dtype=jnp.int32),
    )
    key_all = block_parts[0].reshape(extent, D)
    value_all = block_parts[1].reshape(extent, D)
    grad_content, grad_rel, key_all, value_all = (
        inner_state[0],
        inner_state[1],
        key_all,
        value_all,
    )
    grad_keys, grad_values = (
        lax.psum_scatter(key_all, "tm", scatter_dimension=0, tiled=True),
        lax.psum_scatter(value_all, "tm", scatter_dimension=0, tiled=True),
    )
    half_size = D // 2
    rel_first = grad_rel[..., :half_size]
    rel_second = grad_rel[..., half_size:]
    sine_wide = sine_rows[:, None, :]
    cosine_wide = cosine_rows[:, None, :]
    grad_projected = jnp.concatenate(
        [
            rel_first * sine_wide - rel_second * cosine_wide,
            rel_first * cosine_wide + rel_second * sine_wide,
        ],
        axis=-1,
    ).astype(jnp.bfloat16)
    grad_pos_weight = jnp.einsum(
        "thc,the->che", grad_projected, position_heads, preferred_element_type=jnp.float32
    ).reshape(D, D)
    grad_q_position = jnp.einsum(
        "thc,che->the", grad_projected, pos_heads, preferred_element_type=jnp.float32
    )
    grad_content_bias = jnp.sum(grad_content, axis=0).reshape(D)
    grad_position_bias = jnp.sum(grad_q_position, axis=0).reshape(D)
    grad_query = (grad_content + grad_q_position).reshape(row_count, D).astype(jnp.bfloat16)
    grad_qkv = jnp.concatenate(
        [grad_query, grad_keys.astype(jnp.bfloat16), grad_values.astype(jnp.bfloat16)], axis=1
    )
    grad_qkv_weight = jnp.einsum(
        "tc,tf->cf", attn_norm_low, grad_qkv, preferred_element_type=jnp.float32
    )
    grad_attn_norm = jnp.einsum(
        "tf,cf->tc", grad_qkv, qkv_weight, preferred_element_type=jnp.float32
    )
    grad_from_attn, grad_ln_attn_gain, grad_ln_attn_bias = attn_pull(grad_attn_norm)
    grad_from_mlp, grad_ln_mlp_gain, grad_ln_mlp_bias = mlp_pull(grad_mlp_norm)
    grad_inputs = grad_rows + grad_from_attn + grad_from_mlp
    weight_grads = (
        grad_ln_attn_gain,
        grad_ln_attn_bias,
        grad_ln_mlp_gain,
        grad_ln_mlp_bias,
        grad_qkv_weight,
        grad_content_bias,
        grad_position_bias,
        grad_pos_weight,
        grad_out_weight,
        grad_up_weight,
        grad_up_bias,
        grad_gate_norm_gain,
        grad_gate_norm_bias,
        grad_conv_kernel,
        grad_conv_bias,
        grad_down_weight,
        grad_down_bias,
        grad_merge_weight,
        grad_merge_bias,
    )
    summed = lax.psum(
        (
            weight_grads[0],
            weight_grads[1],
            weight_grads[2],
            weight_grads[3],
            weight_grads[4],
            weight_grads[5],
            weight_grads[6],
            weight_grads[7],
            weight_grads[8],
            weight_grads[9],
            weight_grads[10],
            weight_grads[11],
            weight_grads[12],
            weight_grads[13],
            weight_grads[14],
            weight_grads[15],
            weight_grads[16],
            weight_grads[17],
            weight_grads[18],
        ),
        "tm",
    )
    shares = (
        lax.psum_scatter(
            summed[0].astype(jnp.bfloat16), "stream", scatter_dimension=0, tiled=True
        ).astype(jnp.float32),
        lax.psum_scatter(
            summed[1].astype(jnp.bfloat16), "stream", scatter_dimension=0, tiled=True
        ).astype(jnp.float32),
        lax.psum_scatter(
            summed[2].astype(jnp.bfloat16), "stream", scatter_dimension=0, tiled=True
        ).astype(jnp.float32),
        lax.psum_scatter(
            summed[3].astype(jnp.bfloat16), "stream", scatter_dimension=0, tiled=True
        ).astype(jnp.float32),
        lax.psum_scatter(
            summed[4].astype(jnp.bfloat16), "stream", scatter_dimension=0, tiled=True
        ).astype(jnp.float32),
        lax.psum_scatter(
            summed[5].astype(jnp.bfloat16), "stream", scatter_dimension=0, tiled=True
        ).astype(jnp.float32),
        lax.psum_scatter(
            summed[6].astype(jnp.bfloat16), "stream", scatter_dimension=0, tiled=True
        ).astype(jnp.float32),
        lax.psum_scatter(
            summed[7].astype(jnp.bfloat16), "stream", scatter_dimension=0, tiled=True
        ).astype(jnp.float32),
        lax.psum_scatter(
            summed[8].astype(jnp.bfloat16), "stream", scatter_dimension=0, tiled=True
        ).astype(jnp.float32),
        lax.psum_scatter(
            summed[9].astype(jnp.bfloat16), "stream", scatter_dimension=0, tiled=True
        ).astype(jnp.float32),
        lax.psum_scatter(
            summed[10].astype(jnp.bfloat16), "stream", scatter_dimension=0, tiled=True
        ).astype(jnp.float32),
        lax.psum_scatter(
            summed[11].astype(jnp.bfloat16), "stream", scatter_dimension=0, tiled=True
        ).astype(jnp.float32),
        lax.psum_scatter(
            summed[12].astype(jnp.bfloat16), "stream", scatter_dimension=0, tiled=True
        ).astype(jnp.float32),
        lax.psum_scatter(
            summed[13].astype(jnp.bfloat16), "stream", scatter_dimension=1, tiled=True
        ).astype(jnp.float32),
        lax.psum_scatter(
            summed[14].astype(jnp.bfloat16), "stream", scatter_dimension=0, tiled=True
        ).astype(jnp.float32),
        lax.psum_scatter(
            summed[15].astype(jnp.bfloat16), "stream", scatter_dimension=0, tiled=True
        ).astype(jnp.float32),
        lax.psum_scatter(
            summed[16].astype(jnp.bfloat16), "stream", scatter_dimension=0, tiled=True
        ).astype(jnp.float32),
        lax.psum_scatter(
            summed[17].astype(jnp.bfloat16), "stream", scatter_dimension=0, tiled=True
        ).astype(jnp.float32),
        lax.psum_scatter(
            summed[18].astype(jnp.bfloat16), "stream", scatter_dimension=0, tiled=True
        ).astype(jnp.float32),
    )
    return (out_rows, grad_inputs[None]) + tuple(shares)


LANES = 128
LOW = LANES // 2
BLOCK = 128
TALL = 256
WINDOW = 64
MARGIN = 16
BOUNDS = 16
MEGA = 1024 * 1024
F32 = jnp.float32
BF16 = jnp.bfloat16


def dot_nn(left, right):
    return jnp.dot(left, right, preferred_element_type=F32)


def dot_nt(left, right):
    return lax.dot_general(left, right, (((1,), (1,)), ((), ())), preferred_element_type=F32)


def dot_tn(left, right):
    return lax.dot_general(left, right, (((0,), (0,)), ((), ())), preferred_element_type=F32)


def rows_of(index, size, base=0):
    return pl.ds(pl.multiple_of(index * size, size) + base, size)


def line_of(ref):
    return ref[...].astype(F32).reshape(1, ref.shape[0])


def fold_rows(values):
    return jnp.sum(values.reshape(values.shape[0] // 8, 8, values.shape[1]), axis=0)


def one_row(values):
    return jnp.sum(values, axis=0, keepdims=True)


def turn(values):
    return pltpu.roll(values, LOW, 1)


def low_lanes(rows):
    return lax.broadcasted_iota(jnp.int32, (rows, LANES), 1) < LOW


def centre_rows(inputs):
    mean = jnp.mean(inputs, axis=-1, keepdims=True)
    centred = inputs - mean
    spread = jnp.mean(centred * centred, axis=-1, keepdims=True)
    return centred * lax.rsqrt(spread + EPS)


def gelu_parts(values):
    phi = 0.5 + 0.5 * lax.erf(values * math.sqrt(0.5))
    bell = jnp.exp(values * values * -0.5)
    return values * phi, phi + values * bell * (1.0 / math.sqrt(2.0 * math.pi))


class Part:
    def __init__(self, shape=None, pairs=None, refs=1, late=False):
        self.shape, self.pairs, self.refs, self.late = shape, pairs, refs, late

    def buffer(self, operand):
        return self.shape or operand.shape

    def copies(self, refs, buffer):
        return self.pairs(refs, buffer) if self.pairs else [(refs[0], buffer)]


def blocks_part(late=False):
    def pairs(refs, buffer):
        place = lax.axis_index("tm")
        return [
            (ref, buffer.at[rows_of(lax.bitwise_xor(jnp.int32(apart), place), BLOCK)])
            for apart, ref in enumerate(refs)
        ]

    return Part((HEADS * BLOCK, D), pairs, HEADS, late)


def rows_part(first, size, late=False):
    return Part((size, D), lambda refs, buffer: [(refs[0].at[pl.ds(first, size)], buffer)], late=late)


class Fetch:
    def __init__(self, pairs, buffer, sems, first):
        self.buffer, self.begun = buffer, False
        self.pending = [
            pltpu.make_async_copy(source, target, sems.at[first + index])
            for index, (source, target) in enumerate(pairs)
        ]

    def begin(self):
        if not self.begun:
            for copy in self.pending:
                copy.start()
        self.begun = True

    def __call__(self):
        self.begin()
        for copy in self.pending:
            copy.wait()
        self.pending = []
        return self.buffer


def begin(*fetches):
    for fetch in fetches:
        fetch.begin()


class Send:
    def __init__(self, buffer, target, sems):
        self.buffer, self.target, self.sems, self.copies = buffer, target, sems, []

    def go(self, *index):
        source, target = (self.buffer.at[index], self.target.at[index]) if index else (self.buffer, self.target)
        copy = pltpu.make_async_copy(source, target, self.sems[len(self.copies)])
        copy.start()
        self.copies.append(copy)

    def finish(self):
        if not self.copies:
            self.go()


SPACES = {"v": pltpu.VMEM, "s": pltpu.SMEM, "k": pl.ANY}


def kernel_call(body, out_shapes, plan, scratch=(), megas=58, bounds=False, aliases=None):
    def call(*operands):
        in_specs, buffers, at = [], [], 0
        for item in plan:
            if item == "f":
                in_specs.append(pl.BlockSpec(memory_space=pl.ANY))
                buffers.append(pltpu.VMEM(operands[at].shape, operands[at].dtype))
                at += 1
            elif isinstance(item, Part):
                in_specs += [pl.BlockSpec(memory_space=pl.ANY)] * item.refs
                buffers.append(pltpu.VMEM(item.buffer(operands[at]), operands[at].dtype))
                at += item.refs
            else:
                in_specs.append(pl.BlockSpec(memory_space=SPACES[item]))
                at += 1
        sent = [out for out in out_shapes if len(out) > 2]
        buffers += [pltpu.VMEM(out[3] if len(out) > 3 else out[0], out[1]) for out in sent]
        sem_count = 96
        extra = [pltpu.SMEM((BOUNDS,), jnp.int32)] if bounds else []

        def outer(*refs):
            inputs, rest = refs[: len(in_specs)], refs[len(in_specs) :]
            outputs, rest = rest[: len(out_shapes)], rest[len(out_shapes) :]
            held, rest = list(rest[: len(buffers)]), rest[len(buffers) :]
            sems, rest = rest[0], rest[1:]
            given, at, used = [], 0, 0
            for item in plan:
                if item == "f":
                    given.append(Fetch([(inputs[at], held[0])], held.pop(0), sems, used))
                    given[-1].begin()
                    used += 1
                    at += 1
                elif isinstance(item, Part):
                    buffer = held.pop(0)
                    pairs = item.copies(inputs[at : at + item.refs], buffer)
                    given.append(Fetch(pairs, buffer, sems, used))
                    if not item.late:
                        given[-1].begin()
                    used += len(pairs)
                    at += item.refs
                else:
                    given.append(inputs[at])
                    at += 1
            results = []
            for out, ref in zip(out_shapes, outputs):
                if len(out) > 2:
                    target = out[4](ref) if len(out) > 3 else ref
                    results.append(Send(held.pop(0), target, [sems.at[used + index] for index in range(4)]))
                    used += 4
                else:
                    results.append(ref)
            assert used <= sem_count
            given = [item() if kind == "f" else item for kind, item in zip(plan, given)]
            body(*given, *results, *rest)
            for item in given:
                if isinstance(item, Fetch):
                    item()
            sends = [item for item in results if isinstance(item, Send)]
            for item in sends:
                item.finish()
            for item in sends:
                for copy in item.copies:
                    copy.wait()

        return pl.pallas_call(
            outer,
            out_shape=[jax.ShapeDtypeStruct(out[0], out[1]) for out in out_shapes],
            in_specs=in_specs,
            out_specs=[pl.BlockSpec(memory_space=pl.ANY if len(out) > 2 else pltpu.VMEM) for out in out_shapes],
            scratch_shapes=buffers
            + [pltpu.SemaphoreType.DMA((sem_count,))]
            + [pltpu.VMEM(shape, kind) for shape, kind in scratch]
            + extra,
            input_output_aliases=aliases or {},
            compiler_params=pltpu.CompilerParams(vmem_limit_bytes=megas * MEGA),
            cost_estimate=pl.CostEstimate(flops=0, bytes_accessed=0, transcendentals=0),
        )(*operands)

    return call


def fill_bounds(lengths_ref, bounds_s, total):
    bounds_s[0] = jnp.int32(0)
    end = jnp.int32(0)
    for item in range(ITEMS):
        end = end + lengths_ref[0, item]
        bounds_s[item + 1] = end
    for item in range(ITEMS + 1, BOUNDS):
        bounds_s[item] = jnp.int32(total)


def select_kernel(
    up_ref,
    up_bias_ref,
    gain_ref,
    bias_ref,
    conv_bias_ref,
    taps_ref,
    qkv_ref,
    pos_ref,
    content_ref,
    position_ref,
    up_out,
    table_out,
    qkv_out,
    pos_out,
    bias_out,
):
    place = lax.axis_index("tm")
    quarters = lax.axis_size("stream")
    share = HALF // (quarters * lax.axis_size("tm"))
    lane = lax.broadcasted_iota(jnp.int32, (1, 2 * LANES), 1)
    channel = jnp.where(lane < LANES + LOW, lane, lane - LOW)
    group = jnp.zeros_like(channel)
    for quarter in range(1, quarters):
        group = group + (channel >= quarter * share).astype(jnp.int32)
    source = group * (HALF // quarters) + share * place + channel - group * share
    chosen = (lax.broadcasted_iota(jnp.int32, (HALF, 2 * LANES), 0) == source).astype(F32).astype(BF16)
    gate = dot_nn(up_ref[:, :HALF], chosen)
    conv = dot_nn(up_ref[:, HALF:], chosen)
    up_out[:, :LANES] = gate[:, :LANES].astype(BF16)
    up_out[:, LANES : 2 * LANES] = jnp.where(low_lanes(D), gate[:, LANES:], conv[:, LANES:]).astype(BF16)
    up_out[:, 2 * LANES :] = conv[:, :LANES].astype(BF16)
    up_bias = line_of(up_bias_ref)
    lines = jnp.concatenate(
        [
            up_bias[:, :HALF],
            up_bias[:, HALF:],
            line_of(gain_ref),
            line_of(bias_ref),
            line_of(conv_bias_ref),
            jnp.zeros((3, HALF), F32),
        ],
        axis=0,
    )
    lines = dot_nn(lines.astype(BF16), chosen)
    taps = dot_nn(taps_ref[...], chosen)
    for part in range(2):
        lanes = slice(part * LANES, (part + 1) * LANES)
        table_out[part, :8] = lines[:, lanes]
        table_out[part, 8 : 8 + KERNEL] = taps[:, lanes]
        table_out[part, 8 + KERNEL :] = jnp.zeros((1, LANES), F32)

    odd = lax.rem(place, 2) == 1

    def head_lanes(ref, base):
        at = pl.ds(pl.multiple_of(lax.div(place, 2) * LANES + base, LANES), LANES)
        values = ref[:, at].astype(F32)
        values = jnp.where(odd, turn(values), values)
        return jnp.where(low_lanes(values.shape[0]), values, 0.0)

    for part in range(3):
        qkv_out[:, part * LANES : (part + 1) * LANES] = head_lanes(qkv_ref, part * D).astype(BF16)
    pos_out[...] = head_lanes(pos_ref, 0).astype(BF16)
    bias_out[...] = jnp.zeros((8, LANES), F32)
    for line, ref in enumerate((content_ref, position_ref)):
        values = line_of(ref)
        picked = values[:, :LANES]
        for tile in range(1, D // LANES):
            picked = jnp.where(
                lax.div(place, 2) == tile, values[:, tile * LANES : (tile + 1) * LANES], picked
            )
        picked = jnp.where(odd, turn(picked), picked)
        bias_out[line : line + 1] = jnp.where(low_lanes(1), picked, 0.0)


def angle_rows(coarse_ref, fine_ref, block, rows):
    half = D // 2
    base = coarse_ref[pl.ds(block, 1)]
    base_sine, base_cosine = base[:, :half], base[:, half:]
    sine, cosine = fine_ref[rows, :half], fine_ref[rows, half:]
    return base_sine * cosine + base_cosine * sine, base_cosine * cosine - base_sine * sine


def item_codes(bounds_s, index):
    code = jnp.zeros_like(index)
    for item in range(1, ITEMS + 1):
        code = code + (index >= bounds_s[item]).astype(jnp.int32)
    return jnp.where(code < ITEMS, code, ITEMS + index)


def attend_kernel(
    lengths_ref,
    x_ref,
    attn_gain_ref,
    attn_bias_ref,
    mlp_gain_ref,
    mlp_bias_ref,
    qkv_ref,
    pos_ref,
    bias_ref,
    coarse_ref,
    fine_ref,
    up_ref,
    up_bias_ref,
    n_attn_out,
    n_mlp_out,
    hat_out,
    q_position_out,
    query_out,
    key_out,
    value_out,
    prob_out,
    attn_out,
    stats_out,
    bounds_s,
):
    frames = n_attn_out.buffer.shape[0]
    half = D // 2
    fill_bounds(lengths_ref, bounds_s, frames)
    attn_gain, attn_bias = line_of(attn_gain_ref), line_of(attn_bias_ref)
    mlp_gain, mlp_bias = line_of(mlp_gain_ref), line_of(mlp_bias_ref)
    content, position = bias_ref[0:1], bias_ref[1:2]
    x_ref = x_ref()
    begin(up_ref)

    @pl.loop(0, frames // TALL, unroll=4)
    def _(block):
        rows = rows_of(block, TALL)
        for part in range(TALL // 32):
            at = pl.ds(pl.multiple_of(block * TALL + part * 32, 32), 32)
            hat = centre_rows(x_ref[at].astype(F32))
            hat_out.buffer[at] = hat.astype(BF16)
            n_attn_out.buffer[at] = (hat * attn_gain + attn_bias).astype(BF16)
            n_mlp_out.buffer[at] = (hat * mlp_gain + mlp_bias).astype(BF16)
        parts = dot_nn(n_attn_out.buffer[rows], qkv_ref[...])
        query = parts[:, :LANES]
        query_out.buffer[rows, :LANES] = ((query + content).astype(BF16).astype(F32) * 0.125).astype(BF16)
        q_position = (query + position).astype(BF16)
        q_position_out.buffer[rows] = q_position
        key_out.buffer[rows, :LANES] = parts[:, LANES : 2 * LANES].astype(BF16)
        value_out.buffer[rows] = parts[:, 2 * LANES :].astype(BF16)
        projected = dot_nt(q_position, pos_ref[...])
        for part in range(TALL // 32):
            at = pl.ds(pl.multiple_of(block * TALL + part * 32, 32), 32)
            inner = part * 32 % BLOCK
            sine, cosine = angle_rows(
                coarse_ref, fine_ref, block * (TALL // BLOCK) + part * 32 // BLOCK, slice(inner, inner + 32)
            )
            first = projected[part * 32 : part * 32 + 32, :half]
            second = projected[part * 32 : part * 32 + 32, half:]
            query_out.buffer[at, LANES : LANES + half] = ((first * sine + second * cosine) * 0.125).astype(BF16)
            query_out.buffer[at, LANES + half :] = ((second * sine - first * cosine) * 0.125).astype(BF16)
            key_out.buffer[at, LANES : LANES + half] = cosine.astype(BF16)
            key_out.buffer[at, LANES + half :] = sine.astype(BF16)

    for out in (n_attn_out, n_mlp_out, hat_out, q_position_out, query_out, key_out, value_out):
        out.go()
    up_ref = up_ref()
    up_bias = line_of(up_bias_ref)[:, HALF:]
    lane = lax.broadcasted_iota(jnp.int32, (16, LANES), 1)

    @pl.loop(0, frames // TALL, unroll=2)
    def _(block):
        values = dot_nn(n_mlp_out.buffer[rows_of(block, TALL)], up_ref[...])
        for part in range(TALL // 16):
            pre = values[part * 16 : part * 16 + 16] + up_bias
            hidden = pre * (0.5 + 0.5 * lax.erf(pre * math.sqrt(0.5)))
            mean = jnp.mean(hidden, axis=-1, keepdims=True)
            centred = hidden - mean
            rate = lax.rsqrt(jnp.mean(centred * centred, axis=-1, keepdims=True) + EPS)
            at = pl.ds(pl.multiple_of(block * TALL + part * 16, 16), 16)
            stats_out.buffer[at] = jnp.where(lane == 0, mean, rate)

    stats_out.go()
    key_code = item_codes(bounds_s, lax.broadcasted_iota(jnp.int32, (1, frames), 1))

    low = low_lanes(32)
    for block in range(frames // TALL):
        rows = pl.ds(block * TALL, TALL)
        raw = dot_nt(query_out.buffer[rows], key_out.buffer[...])
        shares = []
        for part in range(TALL // 32):
            start = block * TALL + part * 32
            index = start + lax.broadcasted_iota(jnp.int32, (32, 1), 0)
            scaled = jnp.where(
                item_codes(bounds_s, index) == key_code, raw[part * 32 : part * 32 + 32], MASKED
            )
            weight = jnp.exp(scaled - jnp.max(scaled, axis=1, keepdims=True))
            prob_out.buffer[pl.ds(start, 32)] = weight.astype(BF16)
            shares.append(1.0 / jnp.sum(weight, axis=1, keepdims=True))
        prob_out.go(rows)
        attn = dot_nn(prob_out.buffer[rows], value_out.buffer[...])
        for part in range(TALL // 32):
            share = shares[part]
            attn_out.buffer[pl.ds(block * TALL + part * 32, 32)] = jnp.where(
                low, attn[part * 32 : part * 32 + 32] * share, share
            )


def fill_margins(wide_s, frames):
    edge = jnp.zeros((MARGIN, LANES), F32)
    wide_s[:MARGIN] = edge
    wide_s[MARGIN + frames : 2 * MARGIN + frames] = edge
    base = frames + 3 * MARGIN
    after = base + frames // 2
    low = low_lanes(MARGIN)
    wide_s[base - MARGIN : base] = jnp.where(low, 0.0, turn(wide_s[after - MARGIN : after]))
    wide_s[after : after + MARGIN] = jnp.where(low, turn(wide_s[base : base + MARGIN]), 0.0)


def item_span(bounds_s, frame):
    begin, end = bounds_s[0], bounds_s[BOUNDS - 1]
    for item in range(1, ITEMS + 1):
        edge = bounds_s[item]
        begin = jnp.where(frame >= edge, edge, begin)
    for item in range(ITEMS, 0, -1):
        edge = bounds_s[item]
        end = jnp.where(frame < edge, edge, end)
    return begin, end


def is_whole(bounds_s, start):
    begin, end = item_span(bounds_s, start)
    reach = KERNEL // 2
    low = (begin == 0) | (begin <= start - reach)
    high = (end == bounds_s[BOUNDS - 1]) | (end >= start + WINDOW + reach)
    return low & high & (end >= start + WINDOW)


def tap_limits(bounds_s, start):
    frame = start + lax.broadcasted_iota(jnp.int32, (WINDOW, LANES), 0)
    begin, end = item_span(bounds_s, frame)
    return begin - frame, end - frame


def grouped(values):
    return values.reshape(WINDOW // 8, 8, LANES)


def triple_places(step, frames):
    half = frames // 2
    return (
        pl.multiple_of(step * WINDOW, 2 * MARGIN),
        pl.multiple_of(step * WINDOW + half, 2 * MARGIN),
        pl.multiple_of(step * WINDOW + frames + 2 * MARGIN, 2 * MARGIN),
    )


def over_windows(bounds_s, frames, body):
    half = frames // 2

    @pl.loop(0, half // WINDOW)
    def _(step):
        start = step * WINDOW
        whole = is_whole(bounds_s, start) & is_whole(bounds_s, start + half)

        @pl.when(whole)
        def _():
            body(step, None)

        @pl.when(jnp.logical_not(whole))
        def _():
            first, second = tap_limits(bounds_s, start), tap_limits(bounds_s, start + half)
            low = low_lanes(WINDOW)
            rest = [jnp.where(low, one, other) for one, other in zip(first, second)]
            body(step, (first, second, rest))


def tap_view(window_ref, tap, limits):
    view = window_ref[tap + 1 : tap + 1 + WINDOW]
    if limits is not None:
        shift = tap - KERNEL // 2
        view = jnp.where((limits[0] <= shift) & (limits[1] > shift), view, 0.0)
    return grouped(view)


def mlp_first_kernel(
    lengths_ref,
    n_ref,
    up_ref,
    table_ref,
    stats_ref,
    cot_ref,
    merge_ref,
    down_ref,
    attn_ref,
    mixed_out,
    gate_pre_out,
    grad_out,
    rate_out,
    hat_out,
    early_out,
    vectors_out,
    lines_out,
    hat_s,
    slope_s,
    gate_s,
    hidden_s,
    gate_slope_s,
    conv_s,
    grad_s,
    out_s,
    back_s,
    branch_s,
    mix_s,
    taps_s,
    turn_s,
    tap_sum_s,
    columns_s,
    forward_s,
    backward_s,
    bounds_s,
):
    frames = mix_s.shape[0]
    half = frames // 2
    blocks = frames // BLOCK
    quarters, early_rows, _ = early_out.buffer.shape
    share = early_rows // 8
    channels = quarters * share
    fill_bounds(lengths_ref, bounds_s, frames)
    for part in range(2):
        for tap in range(KERNEL):
            line = jnp.broadcast_to(table_ref[part, 8 + tap : 9 + tap], (8, LANES))
            taps_s[part, tap] = line
            turn_s[part, KERNEL - 1 - tap] = line
    tap_sum_s[...] = jnp.zeros(tap_sum_s.shape, F32)
    main, rest = table_ref[0, :8], table_ref[1, :8]
    mixed_bias = jnp.where(low_lanes(1), rest[0:1], rest[1:2])
    low = low_lanes(64)
    gate_pre_ref = gate_pre_out.buffer
    n_ref = n_ref()
    stats_ref = stats_ref()
    begin(cot_ref, merge_ref, down_ref, attn_ref)

    def stat_rows(rows):
        stats = stats_ref[rows]
        return stats[:, 0:1], stats[:, 1:2]

    def chunk(start, base=0):
        return pl.ds(pl.multiple_of(start, 64) + base, 64)

    def conv_part(hidden, mean, rate, lines, rows, to_rows):
        hat = (hidden - mean) * rate
        hat_s[rows] = hat
        hat_out.buffer[rows] = hat.astype(BF16)
        conv_s[to_rows] = (hat * lines[2:3] + lines[3:4]).astype(BF16).astype(F32)

    @pl.loop(0, half // TALL, unroll=2)
    def _(block):
        pre = [dot_nn(n_ref[rows_of(block, TALL, base)], up_ref[...]) for base in (0, half)]
        for part in range(TALL // 64):
            inner = slice(part * 64, part * 64 + 64)
            start = block * TALL + part * 64
            mixed = []
            for values, base in zip(pre, (0, half)):
                rows = chunk(start, base)
                gate, gate_slope = gelu_parts(values[inner, :LANES] + main[0:1])
                hidden_s[rows] = gate
                gate_slope_s[rows] = gate_slope
                hidden, slope = gelu_parts(values[inner, 2 * LANES :] + main[1:2])
                mean, rate = stat_rows(rows)
                slope_s[rows] = slope * rate
                conv_part(hidden, mean, rate, main, rows, chunk(start, base + MARGIN))
                mixed.append((*gelu_parts(values[inner, LANES : 2 * LANES] + mixed_bias), mean, rate))
            (low_hidden, low_slope, low_mean, low_rate), (high_hidden, high_slope, high_mean, high_rate) = mixed
            rows = chunk(start, frames)
            hidden_s[rows] = jnp.where(low, low_hidden, turn(high_hidden))
            gate_slope_s[rows] = jnp.where(low, low_slope, turn(high_slope))
            rate = jnp.where(low, low_rate, high_rate)
            slope_s[rows] = jnp.where(low, turn(low_slope), high_slope) * rate
            conv_part(
                jnp.where(low, turn(low_hidden), high_hidden),
                jnp.where(low, low_mean, high_mean),
                rate,
                rest,
                rows,
                chunk(start, frames + 3 * MARGIN),
            )

    hat_out.go()
    fill_margins(conv_s, frames)
    tall = WINDOW + 2 * MARGIN
    outs = (0, half, frames)

    def convolve(step, limits):
        for index, base in enumerate(triple_places(step, frames)):
            forward_s[index] = conv_s[pl.ds(base, tall)]
        for index in range(3):
            own = None if limits is None else limits[index]
            total = jnp.zeros((WINDOW // 8, 8, LANES), F32)
            for tap in range(KERNEL):
                total = total + tap_view(forward_s.at[index], tap, own) * taps_s[index // 2, tap][None]
            lines = rest if index == 2 else main
            out_s[rows_of(step, WINDOW, outs[index])] = total.reshape(WINDOW, LANES) + lines[4:5]

    over_windows(bounds_s, frames, convolve)
    cot_ref = cot_ref()
    merge_ref = merge_ref()
    down_ref = down_ref()
    attn_ref = attn_ref()
    down_ref[channels:] = jnp.zeros((2 * LANES - channels, D), BF16)
    zero = jnp.zeros((8, LANES), F32)

    def branch_part(grad_gated, rows, to_rows, sums):
        up_sum, conv_sum = sums
        gate, conv = hidden_s[rows], out_s[rows]
        gate_pre = (grad_gated * conv * gate_slope_s[rows]).astype(BF16)
        gate_pre_ref[rows] = gate_pre
        grad_conv = (grad_gated * gate).astype(BF16).astype(F32)
        grad_s[to_rows] = grad_conv
        gate_pre = gate_pre.astype(F32)
        return gate * conv, gate_pre, (up_sum + fold_rows(gate_pre), conv_sum + fold_rows(grad_conv))

    def branch_step(block, sums):
        main_sums, rest_sums = sums
        grads = []
        for base in (0, half):
            rows = rows_of(block, TALL, base)
            branch = dot_nt(cot_ref[rows], merge_ref[...]).astype(BF16)
            branch_s[rows] = branch
            grads.append(dot_nt(branch, down_ref[...]))
        for part in range(TALL // 64):
            inner = slice(part * 64, part * 64 + 64)
            start = block * TALL + part * 64
            for values, base in zip(grads, (0, half)):
                rows = chunk(start, base)
                gated, gate_pre, main_sums = branch_part(
                    values[inner, :LANES], rows, chunk(start, base + MARGIN), main_sums
                )
                mix_s[rows, :LANES] = gated.astype(BF16)
                gate_s[rows, :LANES] = gate_pre.astype(BF16)
            grad = jnp.where(low, grads[0][inner, LANES:], turn(grads[1][inner, LANES:]))
            gated, gate_pre, rest_sums = branch_part(
                grad, chunk(start, frames), chunk(start, frames + 3 * MARGIN), rest_sums
            )
            low_rows, high_rows = chunk(start), chunk(start, half)
            gate_s[low_rows, LANES:] = gate_pre.astype(BF16)
            gate_s[high_rows, LANES:] = turn(gate_pre).astype(BF16)
            mix_s[low_rows, LANES:] = jnp.where(low, gated, turn(attn_ref[low_rows])).astype(BF16)
            mix_s[high_rows, LANES:] = jnp.where(low, turn(gated), turn(attn_ref[high_rows])).astype(BF16)
        return main_sums, rest_sums

    (main_up, main_conv), (rest_up, rest_conv) = lax.fori_loop(
        0, half // TALL, branch_step, ((zero, zero), (zero, zero)), unroll=2
    )
    gate_pre_out.go()
    fill_margins(grad_s, frames)
    ones = jnp.ones((16, frames), BF16)
    lines_out[0:1] = dot_nn(ones, branch_s[...])[0:1]
    lines_out[1:2] = dot_nn(ones, cot_ref[...])[0:1]
    lines_out[2:8] = jnp.zeros((6, D), F32)
    grad_down = dot_tn(mix_s[...], branch_s[...])
    grad_gate = dot_tn(gate_s[...], n_ref[...])
    for quarter in range(quarters):
        for tile in range(4):
            early_out.buffer[quarter, tile * share : (tile + 1) * share] = grad_down[
                quarter * share : (quarter + 1) * share, tile * LANES : (tile + 1) * LANES
            ].astype(BF16)
        early_out.buffer[quarter, 4 * share :] = grad_gate[
            :channels, quarter * LANES : (quarter + 1) * LANES
        ].astype(BF16)
    early_out.go()
    for block in range(blocks):
        mixed_out.buffer[block, :BLOCK] = mix_s[block * BLOCK : (block + 1) * BLOCK]
    mixed_out.go(slice(None), pl.ds(0, BLOCK))

    def differentiate(step, limits):
        for index, base in enumerate(triple_places(step, frames)):
            forward_s[index] = conv_s[pl.ds(base, tall)]
            backward_s[index] = grad_s[pl.ds(base, tall)]
        for index in range(3):
            own = None if limits is None else limits[index]
            total = jnp.zeros((WINDOW // 8, 8, LANES), F32)
            centre = grouped(backward_s[index, MARGIN : MARGIN + WINDOW])
            for tap in range(KERNEL):
                total = total + tap_view(backward_s.at[index], tap, own) * turn_s[index // 2, tap][None]
                tap_sum_s[index // 2, tap] += jnp.sum(tap_view(forward_s.at[index], tap, own) * centre, axis=0)
            back_s[rows_of(step, WINDOW, outs[index])] = total.reshape(WINDOW, LANES)

    over_windows(bounds_s, frames, differentiate)
    lane = lax.broadcasted_iota(jnp.int32, (64, LANES), 1)

    def norm_part(rows, lines, sums):
        gain_sum, bias_sum = sums
        back, hat, slope = back_s[rows], hat_s[rows], slope_s[rows]
        grad = back * lines[2:3]
        grad_out.buffer[rows] = (grad * slope).astype(BF16)
        rate_out.buffer[rows] = slope.astype(BF16)
        along = back * hat
        return grad, along * lines[2:3], (gain_sum + fold_rows(along), bias_sum + fold_rows(back))

    def norm_step(block, sums):
        main_sums, rest_sums = sums
        for part in range(TALL // 64):
            start = block * TALL + part * 64
            pairs = []
            for base in (0, half):
                plain, along, main_sums = norm_part(chunk(start, base), main, main_sums)
                pairs.append([plain, along])
            plain, along, rest_sums = norm_part(chunk(start, frames), rest, rest_sums)
            for item, values in enumerate((plain, along)):
                pairs[0][item] = pairs[0][item] + jnp.where(low, values, 0.0)
                pairs[1][item] = pairs[1][item] + jnp.where(low, 0.0, values)
            for (plain, along), base in zip(pairs, (0, half)):
                columns_s[chunk(start, base)] = jnp.where(
                    lane == 0,
                    jnp.sum(plain, axis=-1, keepdims=True),
                    jnp.where(lane == 1, jnp.sum(along, axis=-1, keepdims=True), 0.0),
                )
        return main_sums, rest_sums

    (main_gain, main_bias), (rest_gain, rest_bias) = lax.fori_loop(
        0, half // TALL, norm_step, ((zero, zero), (zero, zero)), unroll=2
    )
    grad_out.go()
    rate_out.go()
    totals = jnp.concatenate(
        [jnp.transpose(columns_s[block * BLOCK : (block + 1) * BLOCK])[:2] for block in range(blocks)], axis=0
    )
    high = totals.astype(BF16)
    low_part = (totals - high.astype(F32)).astype(BF16)
    for block in range(blocks):
        mixed_out.buffer[block, BLOCK:, :LANES] = high
        mixed_out.buffer[block, BLOCK:, LANES:] = low_part
    mixed_out.go(slice(None), pl.ds(BLOCK, 2 * blocks))

    def vectors(part, lines):
        taps = jnp.sum(tap_sum_s[part], axis=1)[:KERNEL]
        stacked = jnp.concatenate([taps] + [one_row(line) for line in lines], axis=0)
        if part:
            stacked = stacked + turn(stacked)
        return jnp.transpose(
            jnp.concatenate([stacked, jnp.zeros((LANES - stacked.shape[0], LANES), F32)], axis=0)
        )

    vectors_out[:LANES] = vectors(0, (main_conv, main_gain, main_bias, main_up))
    vectors_out[LANES:] = vectors(1, (rest_conv, rest_gain, rest_bias, rest_up))[: channels - LANES]


def attend_back_kernel(
    cot_ref,
    merge_ref,
    head_ref,
    attn_ref,
    value_ref,
    prob_ref,
    key_ref,
    coarse_ref,
    fine_ref,
    pos_ref,
    query_ref,
    n_ref,
    q_position_ref,
    qkv_ref,
    hat_ref,
    gain_ref,
    early_ref,
    branch_out,
    total_out,
    pack_0,
    pack_1,
    pack_2,
    pack_3,
    lines_out,
    grad_s,
    raw_s,
    projected_s,
    parts_s,
    grads_s,
):
    place = lax.axis_index("tm")
    frames = raw_s.shape[0]
    blocks = frames // BLOCK
    half = D // 2
    zero = jnp.zeros((8, LANES), F32)
    cot_ref, merge_ref, head_ref, attn_ref = cot_ref(), merge_ref(), head_ref(), attn_ref()
    head_ref[HEAD:] = jnp.zeros((LANES - HEAD, D), BF16)
    begin(value_ref, prob_ref, key_ref, pos_ref)

    @pl.loop(0, frames // TALL, unroll=4)
    def _(block):
        rows = rows_of(block, TALL)
        branch = dot_nt(cot_ref[rows], merge_ref[...]).astype(BF16)
        branch_out.buffer[rows] = branch
        grad_s[rows] = (dot_nt(branch, head_ref[...]) * attn_ref[rows, HEAD : HEAD + 1]).astype(BF16)

    branch_out.go()
    value_ref, prob_ref = value_ref(), prob_ref()
    key_ref, pos_ref = key_ref(), pos_ref()
    begin(query_ref, n_ref, q_position_ref, qkv_ref, hat_ref, early_ref)

    def score_step(block, sums):
        content_sum, position_sum = sums
        rows = rows_of(block, TALL)
        grad = grad_s[rows]
        score = dot_nt(grad, value_ref[...])
        for part in range(TALL // 32):
            at = pl.ds(pl.multiple_of(block * TALL + part * 32, 32), 32)
            inner = slice(part * 32, part * 32 + 32)
            delta = jnp.sum(grad[inner].astype(F32) * attn_ref[at], axis=1, keepdims=True)
            raw_s[at] = (prob_ref[at].astype(F32) * (score[inner] - delta)).astype(BF16)
        query = dot_nn(raw_s[rows], key_ref[...]) * 0.125
        for part in range(TALL // 32):
            at = pl.ds(pl.multiple_of(block * TALL + part * 32, 32), 32)
            inner = part * 32 % BLOCK
            sine, cosine = angle_rows(
                coarse_ref, fine_ref, block * (TALL // BLOCK) + part * 32 // BLOCK, slice(inner, inner + 32)
            )
            inner = slice(part * 32, part * 32 + 32)
            first, second = query[inner, LANES : LANES + half], query[inner, LANES + half :]
            projected_s[at, :half] = (first * sine - second * cosine).astype(BF16)
            projected_s[at, half:] = (first * cosine + second * sine).astype(BF16)
        position = dot_nn(projected_s[rows], pos_ref[...])
        content = query[:, :LANES]
        parts_s[rows, :LANES] = (content + position).astype(BF16)
        return content_sum + fold_rows(content), position_sum + fold_rows(position)

    content_sum, position_sum = lax.fori_loop(0, frames // TALL, score_step, (zero, zero), unroll=4)
    query_ref, n_ref, q_position_ref = query_ref(), n_ref(), q_position_ref()
    qkv_ref, hat_ref = qkv_ref(), hat_ref()
    grad_key = dot_tn(query_ref[...], raw_s[...])
    grad_value = dot_tn(grad_s[...], prob_ref[...])
    for block in range(blocks):
        at = slice(block * BLOCK, (block + 1) * BLOCK)
        parts_s[at, LANES : 2 * LANES] = jnp.transpose(grad_key[:, at]).astype(BF16)
        parts_s[at, 2 * LANES :] = jnp.transpose(grad_value[:, at]).astype(BF16)
    grads_s[:HEAD] = dot_tn(parts_s[:, :LANES], n_ref[...])[:HEAD]
    grads_s[HEAD : 2 * HEAD] = dot_nn(grad_key.astype(BF16), n_ref[...])[:HEAD]
    grads_s[2 * HEAD : 3 * HEAD] = dot_nn(grad_value.astype(BF16), n_ref[...])[:HEAD]
    grads_s[3 * HEAD :] = dot_tn(q_position_ref[...], projected_s[...])[:HEAD]
    stream = lax.axis_index("stream")
    early_ref = early_ref()
    for apart, pack_out in enumerate((pack_0, pack_1, pack_2, pack_3)):
        quarter = lax.bitwise_xor(stream, jnp.int32(apart))
        lanes = pl.ds(pl.multiple_of(quarter * LANES, LANES), LANES)
        pack_out.buffer[: 4 * HEAD] = grads_s[:, lanes].astype(BF16)
        pack_out.buffer[4 * HEAD :] = early_ref[quarter]
        pack_out.go()
    gain = line_of(gain_ref)
    wide_zero = jnp.zeros((8, D), F32)

    def norm_step(block, sums):
        gain_sum, bias_sum = sums
        grad = dot_nt(parts_s[rows_of(block, TALL)], qkv_ref[...])
        for part in range(TALL // 32):
            at = pl.ds(pl.multiple_of(block * TALL + part * 32, 32), 32)
            own = grad[part * 32 : part * 32 + 32]
            total_out.buffer[at] = (own * gain).astype(BF16)
            gain_sum = gain_sum + fold_rows(own * hat_ref[at].astype(F32))
            bias_sum = bias_sum + fold_rows(own)
        return gain_sum, bias_sum

    gain_sum, bias_sum = lax.fori_loop(0, frames // TALL, norm_step, (wide_zero, wide_zero), unroll=4)
    lane = lax.broadcasted_iota(jnp.int32, (1, LANES), 1)

    def own_lanes(sums):
        line = one_row(sums)
        line = line + turn(line)
        tiles = [
            jnp.where(lax.div(tile * LANES + lane, HEAD) == place, line, 0.0) for tile in range(D // LANES)
        ]
        return jnp.concatenate(tiles, axis=1)

    lines_out[...] = jnp.concatenate(
        [
            one_row(gain_sum),
            one_row(bias_sum),
            own_lanes(content_sum),
            own_lanes(position_sum),
            jnp.zeros((4, D), F32),
        ],
        axis=0,
    )


def mlp_second_kernel(
    mixed_ref,
    gate_pre_ref,
    grad_ref,
    rate_ref,
    hat_ref,
    up_ref,
    norm_hat_ref,
    gain_ref,
    other_ref,
    n_ref,
    vectors_ref,
    first_lines_ref,
    head_lines_ref,
    joined_ref,
    branch_ref,
    cot_ref,
    same_out,
    apart_out,
    pack_out,
    pre_s,
    columns_s,
    grad_up_s,
    lines_s,
    up_columns_s,
    merge_s,
    head_s,
):
    pack_ref = pack_out.buffer
    place = lax.axis_index("tm")
    frames = pre_s.shape[0]
    half = frames // 2
    blocks = frames // BLOCK
    quarters = pack_ref.shape[0]
    channels = vectors_ref.shape[0]
    share = channels // quarters
    totals = jnp.zeros((2 * blocks, LANES), F32)
    mixed_ref = mixed_ref()
    for source in range(mixed_ref.shape[0]):
        both = mixed_ref[source].astype(F32)
        totals = totals + (both[:, :LANES] + both[:, LANES:])
    totals = totals * (1.0 / HALF)
    columns = jnp.transpose(jnp.concatenate([totals, jnp.zeros((LANES - 2 * blocks, LANES), F32)], axis=0))
    lane = lax.broadcasted_iota(jnp.int32, (BLOCK, LANES), 1)
    for block in range(blocks):
        columns_s[block * BLOCK : (block + 1) * BLOCK] = jnp.where(
            lane == 0, columns[:, 2 * block : 2 * block + 1], columns[:, 2 * block + 1 : 2 * block + 2]
        )
    gate_pre_ref, grad_ref, rate_ref, hat_ref = gate_pre_ref(), grad_ref(), rate_ref(), hat_ref()
    begin(n_ref, up_ref, norm_hat_ref, other_ref, joined_ref, branch_ref, cot_ref)
    low = low_lanes(64)
    gain = line_of(gain_ref)

    def chunk(start, base=0):
        return pl.ds(pl.multiple_of(start, 64) + base, 64)

    def pre_part(rows, table, up_sum):
        plain, along = table
        hat, rate = hat_ref[rows].astype(F32), rate_ref[rows].astype(F32)
        pre = (grad_ref[rows].astype(F32) - rate * (plain + hat * along)).astype(BF16).astype(F32)
        return pre, up_sum + fold_rows(pre)

    def pre_step(block, sums):
        main_up, rest_up = sums
        for part in range(TALL // 64):
            start = block * TALL + part * 64
            tables = []
            for base in (0, half):
                rows = chunk(start, base)
                values = columns_s[rows]
                table = [values[:, item : item + 1] for item in range(2)]
                tables.append(table)
                pre, main_up = pre_part(rows, table, main_up)
                pre_s[rows, :LANES] = gate_pre_ref[rows]
                pre_s[rows, 2 * LANES :] = pre.astype(BF16)
            rows = chunk(start, frames)
            table = [jnp.where(low, one, other) for one, other in zip(*tables)]
            pre, rest_up = pre_part(rows, table, rest_up)
            gate_pre = gate_pre_ref[rows].astype(F32)
            pre_s[chunk(start), LANES : 2 * LANES] = jnp.where(low, gate_pre, turn(pre)).astype(BF16)
            pre_s[chunk(start, half), LANES : 2 * LANES] = jnp.where(low, turn(gate_pre), pre).astype(BF16)
        return main_up, rest_up

    zero = jnp.zeros((8, LANES), F32)
    main_up, rest_up = lax.fori_loop(0, half // TALL, pre_step, (zero, zero), unroll=2)
    n_ref, up_ref, norm_hat_ref, other_ref = n_ref(), up_ref(), norm_hat_ref(), other_ref()
    grad_up_s[...] = dot_tn(pre_s[:, LANES:], n_ref[...])
    wide_zero = jnp.zeros((8, D), F32)

    def norm_step(block, sums):
        gain_sum, bias_sum = sums
        rows = rows_of(block, BLOCK)
        grad = dot_nt(pre_s[rows], up_ref[...])
        total = (grad * gain + other_ref[rows].astype(F32)).astype(BF16)
        apart = lax.bitwise_xor(block, place)

        @pl.when(lax.rem(apart, 2) == 0)
        def _():
            same_out.buffer[lax.div(apart, 2)] = total

        @pl.when(lax.rem(apart, 2) == 1)
        def _():
            apart_out.buffer[lax.div(apart, 2)] = total

        return gain_sum + fold_rows(grad * norm_hat_ref[rows].astype(F32)), bias_sum + fold_rows(grad)

    gain_sum, bias_sum = lax.fori_loop(0, blocks, norm_step, (wide_zero, wide_zero), unroll=4)
    apart_out.go()
    same_out.go()
    rest_line = one_row(rest_up)
    up_columns_s[:LANES] = jnp.transpose(jnp.broadcast_to(one_row(main_up), (LANES, LANES)))
    up_columns_s[LANES:] = jnp.transpose(jnp.broadcast_to(rest_line + turn(rest_line), (LANES, LANES)))[:LOW]
    first_device = (place == 0).astype(F32)
    lines_s[...] = jnp.concatenate(
        [
            head_lines_ref[0:2],
            one_row(gain_sum),
            one_row(bias_sum),
            head_lines_ref[2:4],
            first_lines_ref[0:2] * first_device,
            jnp.zeros((8, D), F32),
        ],
        axis=0,
    )
    joined_ref, branch_ref, cot_ref = joined_ref(), branch_ref(), cot_ref()
    sources, _, source_rows = joined_ref.shape
    merge_rows = merge_s.shape[0]
    head_rows = head_s.shape[0]
    grad_merge = jnp.zeros(merge_s.shape, F32)
    grad_head = jnp.zeros(head_s.shape, F32)
    for source in range(sources):
        at = slice(source * source_rows, (source + 1) * source_rows)
        grad_merge = grad_merge + dot_nn(joined_ref[source, :merge_rows], cot_ref[at])
        grad_head = grad_head + dot_nn(joined_ref[source, merge_rows : merge_rows + head_rows], branch_ref[at])
    merge_s[...] = grad_merge
    head_s[...] = grad_head
    gate_at = KERNEL + 3
    lane = lax.broadcasted_iota(jnp.int32, (share, LANES), 1)
    for quarter in range(quarters):
        lanes = slice(quarter * LANES, (quarter + 1) * LANES)
        pack_ref[quarter, :LANES] = grad_up_s[LANES:, lanes].astype(BF16)
        pack_ref[quarter, LANES:channels] = grad_up_s[LOW:LANES, lanes].astype(BF16)
        table = vectors_ref[quarter * share : (quarter + 1) * share]
        for other in range(2):
            at = slice((2 * (quarter % 2) + other) * share, (2 * (quarter % 2) + other + 1) * share)
            column = vectors_ref[at, gate_at : gate_at + 1] if quarter < quarters // 2 else up_columns_s[at, 0:1]
            table = jnp.where(lane == gate_at + other, column, table)
        pack_ref[quarter, channels : channels + share] = table.astype(BF16)
        pack_ref[quarter, channels + share : channels + share + 16] = lines_s[:, lanes].astype(BF16)
        base = channels + share + 16
        for part_s in (merge_s, head_s):
            part_share = part_s.shape[0] // quarters
            at = slice(quarter * part_share, (quarter + 1) * part_share)
            for tile in range(4):
                pack_ref[quarter, base : base + part_share] = part_s[at, tile * LANES : (tile + 1) * LANES].astype(BF16)
                base += part_share


def output_kernel(
    x_ref, mixed_ref, head_ref, down_ref, down_bias_ref, merge_ref, merge_bias_ref, out_ref, joined_out
):
    sources = mixed_ref.shape[0]
    rows = x_ref.shape[0]
    channels = HALF // sources
    share = channels // 4
    attn_parts = []
    branch_attn = jnp.zeros((rows, D), F32)
    branch_mlp = jnp.zeros((rows, D), F32)
    for source in range(sources):
        attn = turn(mixed_ref[source, :rows, LANES:].astype(F32))[:, :HEAD].astype(BF16)
        attn_parts.append(attn)
        branch_attn = branch_attn + dot_nn(attn, head_ref[source * HEAD : (source + 1) * HEAD])
        down = jnp.concatenate(
            [down_ref[(part * sources + source) * share : (part * sources + source + 1) * share] for part in range(4)],
            axis=0,
        )
        branch_mlp = branch_mlp + dot_nn(mixed_ref[source, :rows, :channels], down)
    joined = jnp.concatenate(
        [branch_attn.astype(BF16), (branch_mlp + line_of(down_bias_ref)).astype(BF16)], axis=1
    )
    result = x_ref[...].astype(F32) + dot_nn(joined, merge_ref[...]) + line_of(merge_bias_ref)
    out_ref[...] = result.astype(BF16)
    turned = jnp.transpose(joined.astype(F32))
    heads = jnp.transpose(jnp.concatenate(attn_parts, axis=1).astype(F32))
    merge_share = turned.shape[0] // (4 * sources)
    head_share = heads.shape[0] // (4 * sources)
    used = 4 * (merge_share + head_share)
    for target in range(sources):
        for part in range(4):
            at = (part * sources + target) * merge_share
            joined_out[target, part * merge_share : (part + 1) * merge_share] = turned[
                at : at + merge_share
            ].astype(BF16)
            at = (part * sources + target) * head_share
            to = 4 * merge_share + part * head_share
            joined_out[target, to : to + head_share] = heads[at : at + head_share].astype(BF16)
        joined_out[target, used:] = jnp.zeros((joined_out.shape[1] - used, rows), BF16)


def pair_kernel(same_ref, other_ref, *out_refs):
    for slot, out_ref in enumerate(out_refs):
        out_ref[...] = (same_ref[slot].astype(F32) + other_ref[slot].astype(F32)).astype(BF16)


def frames_kernel(x_ref, cot_ref, *refs):
    total_refs, out_ref = refs[:-1], refs[-1]
    for part in range(x_ref.shape[0] // 32):
        rows = slice(part * 32, part * 32 + 32)
        inputs = x_ref[rows].astype(F32)
        mean = jnp.mean(inputs, axis=-1, keepdims=True)
        centred = inputs - mean
        rate = lax.rsqrt(jnp.mean(centred * centred, axis=-1, keepdims=True) + EPS)
        hat = centred * rate
        grad = total_refs[0][rows].astype(F32)
        for total_ref in total_refs[1:]:
            grad = grad + total_ref[rows].astype(F32)
        plain = jnp.mean(grad, axis=-1, keepdims=True)
        along = jnp.mean(grad * hat, axis=-1, keepdims=True)
        out_ref[rows] = cot_ref[rows].astype(F32) + rate * (grad - plain - hat * along)


def add_kernel(*refs):
    out_ref = refs[-1]
    first = 0
    for at in range(0, len(refs) - 1, 4):
        total = refs[at][...].astype(F32)
        for ref in refs[at + 1 : at + 4]:
            total = total + ref[...].astype(F32)
        out_ref[first : first + total.shape[0]] = total.astype(BF16)
        first += total.shape[0]


def gather_parts(near_ref, far_ref, all_s):
    place = lax.axis_index("tm")
    for apart in range(all_s.shape[0]):
        part_ref = far_ref if apart % 2 else near_ref
        all_s[lax.bitwise_xor(jnp.int32(apart), place)] = part_ref[apart // 2]


def lines_from(all_s, base, size):
    return jnp.concatenate([all_s[source, base : base + size] for source in range(all_s.shape[0])], axis=0).astype(F32)


def add_streams_kernel(parts_ref, out_ref):
    total = parts_ref[0].astype(F32)
    for source in range(1, parts_ref.shape[0]):
        total = total + parts_ref[source].astype(F32)
    out_ref[...] = total.astype(BF16)


def early_kernel(near_ref, far_ref, qkv_out, pos_out, down_out, up_out, all_s):
    gather_parts(near_ref, far_ref, all_s)
    sources = all_s.shape[0]
    share = HALF // (4 * sources)
    for kind in range(4):
        lines = jnp.transpose(lines_from(all_s, kind * HEAD, HEAD))
        if kind < 3:
            qkv_out[:, kind * D : (kind + 1) * D] = lines
        else:
            pos_out[...] = lines
    base = 4 * HEAD
    for source in range(sources):
        for tile in range(4):
            down_out[source * share : (source + 1) * share, tile * LANES : (tile + 1) * LANES] = all_s[
                source, base + tile * share : base + (tile + 1) * share
            ].astype(F32)
    wide = sources * share
    for group in range(4):
        up_out.buffer[:, group * wide : (group + 1) * wide] = jnp.transpose(
            lines_from(all_s, base + 4 * share + group * share, share)
        )


def late_kernel(*refs):
    _, near_ref, far_ref = refs[:3]
    (
        attn_gain_out,
        attn_bias_out,
        mlp_gain_out,
        mlp_bias_out,
        content_out,
        position_out,
        outw_out,
        up_out,
        up_bias_out,
        gain_out,
        bias_out,
        taps_out,
        conv_bias_out,
        down_bias_out,
        merge_out,
        merge_bias_out,
        all_s,
    ) = refs[3:]
    gather_parts(near_ref, far_ref, all_s)
    sources = all_s.shape[0]
    channels = HALF // sources
    share = channels // 4
    base = 0
    for group in range(4):
        at = group * sources * share
        up_out.buffer[:, at : at + sources * share] = jnp.transpose(lines_from(all_s, base + group * share, share))
    up_out.go()
    table = jnp.transpose(lines_from(all_s, base + channels, share))
    taps_out[...] = table[:KERNEL]
    conv_bias_out[...] = table[KERNEL]
    gain_out[...] = table[KERNEL + 1]
    bias_out[...] = table[KERNEL + 2]
    wide = sources * share
    up_bias_out[:wide] = table[KERNEL + 3]
    up_bias_out[wide:] = table[KERNEL + 4]
    base = base + channels + share
    lines = all_s[0, base : base + 16].astype(F32)
    for source in range(1, sources):
        lines = lines + all_s[source, base : base + 16].astype(F32)
    outs = (attn_gain_out, attn_bias_out, mlp_gain_out, mlp_bias_out, content_out, position_out, down_bias_out, merge_bias_out)
    for line, out in enumerate(outs):
        out[...] = lines[line]
    base = base + 16
    merge_share = 2 * D // (4 * sources)
    head_share = D // (4 * sources)
    for source in range(sources):
        for tile in range(4):
            lanes = slice(tile * LANES, (tile + 1) * LANES)
            at = base + tile * merge_share
            merge_out[source * merge_share : (source + 1) * merge_share, lanes] = all_s[
                source, at : at + merge_share
            ].astype(F32)
            at = base + 4 * merge_share + tile * head_share
            outw_out[source * head_share : (source + 1) * head_share, lanes] = all_s[
                source, at : at + head_share
            ].astype(F32)


def moved(block, axis, bits):
    count = lax.axis_size(axis)
    return lax.ppermute(block, axis, [(index, index ^ bits) for index in range(count)])


def over_streams(packs):
    return [packs[0]] + [moved(packs[bits], "stream", bits) for bits in range(1, lax.axis_size("stream"))]


def near_blocks(block):
    return [block] + [moved(block, "tm", bits) for bits in range(2, lax.axis_size("tm"), 2)]


def far_blocks(near):
    far = [moved(part, "tm", 1) for part in near]
    return [part for pair in zip(near, far) for part in pair]


def far_stack(near):
    stack = jnp.stack(near)
    return stack, moved(stack, "tm", 1)


def head_device(
    frames,
    lengths,
    cotangent,
    ln_attn_gain,
    ln_attn_bias,
    ln_mlp_gain,
    ln_mlp_bias,
    qkv_weight,
    content_bias,
    position_bias,
    pos_weight,
    out_weight,
    up_weight,
    up_bias,
    gate_norm_gain,
    gate_norm_bias,
    conv_kernel,
    conv_bias,
    down_weight,
    down_bias,
    merge_weight,
    merge_bias,
):
    count = lax.axis_size("tm")
    quarters = lax.axis_size("stream")
    own = frames.shape[1]
    total = own * count
    folded = total + total // 2
    padded = folded + 4 * MARGIN
    share = HALF // (quarters * count)
    channels = HALF // count
    quarter = D // quarters
    own_frames = frames[0]
    own_cotangent = cotangent[0]

    whole, late = Part(), Part(late=True)
    near = near_blocks(own_frames)
    cot_near = near_blocks(own_cotangent)
    up_own, table, qkv_own, pos_own, bias_own = kernel_call(
        select_kernel,
        [
            ((D, 3 * LANES), BF16),
            ((2, 8 + KERNEL + 1, LANES), F32),
            ((D, 3 * LANES), BF16),
            ((D, LANES), BF16),
            ((8, LANES), F32),
        ],
        10 * "v",
    )(
        up_weight,
        up_bias,
        gate_norm_gain,
        gate_norm_bias,
        conv_bias,
        conv_kernel,
        qkv_weight,
        pos_weight,
        content_bias,
        position_bias,
    )
    near, up_own = lax.optimization_barrier((near, up_own))
    blocks = far_blocks(near)
    frequency = jnp.exp(jnp.arange(D // 2, dtype=F32) * (-2.0 * math.log(10000.0) / D))
    coarse = jnp.arange(0, total, BLOCK, dtype=F32)[:, None] * frequency[None]
    fine = jnp.arange(BLOCK, dtype=F32)[:, None] * frequency[None]
    coarse_table = jnp.concatenate([jnp.sin(coarse), jnp.cos(coarse)], axis=1)
    fine_table = jnp.concatenate([jnp.sin(fine), jnp.cos(fine)], axis=1)

    n_attn, n_mlp, hat, q_position, query, key, value, prob, attn, stats = kernel_call(
        attend_kernel,
        [
            ((total, D), BF16, 1),
            ((total, D), BF16, 1),
            ((total, D), BF16, 1),
            ((total, LANES), BF16, 1),
            ((total, LANES + D), BF16, 1),
            ((total, LANES + D), BF16, 1),
            ((total, LANES), BF16, 1),
            ((total, total), BF16, 1),
            ((total, LANES), F32, 1),
            ((total, LANES), F32, 1),
        ],
        [
            "s",
            blocks_part(),
            *"vvvvvvvvv",
            Part((D, HALF), lambda refs, buffer: [(refs[0].at[:, pl.ds(HALF, HALF)], buffer)], late=True),
            "v",
        ],
        bounds=True,
    )(
        lengths,
        *blocks,
        ln_attn_gain,
        ln_attn_bias,
        ln_mlp_gain,
        ln_mlp_bias,
        qkv_own,
        pos_own,
        bias_own,
        coarse_table,
        fine_table,
        up_weight,
        up_bias,
    )

    n_mlp, cot_near = lax.optimization_barrier((n_mlp, cot_near))
    cot = far_blocks(cot_near)

    def own_down(refs, buffer):
        place = lax.axis_index("tm")
        stride = HALF // quarters
        return [
            (
                refs[0].at[pl.ds(pl.multiple_of(part * stride + share * place, 16), share)],
                buffer.at[pl.ds(part * share, share)],
            )
            for part in range(quarters)
        ]

    mixed, gate_pre, grad_y, slope, gate_hat, early_pack, vectors, first_lines = kernel_call(
        mlp_first_kernel,
        [
            ((count, own + 16, 2 * LANES), BF16, 1),
            ((folded, LANES), BF16, 1),
            ((folded, LANES), BF16, 1),
            ((folded, LANES), BF16, 1),
            ((folded, LANES), BF16, 1),
            ((quarters, 8 * share, LANES), BF16, 1),
            ((channels, LANES), F32),
            ((8, D), F32),
        ],
        [
            "s",
            whole,
            "v",
            "v",
            whole,
            blocks_part(late=True),
            rows_part(D, D, late=True),
            Part((2 * LANES, D), own_down, late=True),
            Part(late=True),
        ],
        [
            ((folded, LANES), F32),
            ((folded, LANES), F32),
            ((total, 2 * LANES), BF16),
            ((folded, LANES), F32),
            ((folded, LANES), F32),
            ((padded, LANES), F32),
            ((padded, LANES), F32),
            ((folded, LANES), F32),
            ((folded, LANES), F32),
            ((total, D), BF16),
            ((total, 2 * LANES), BF16),
            ((2, 32, 8, LANES), F32),
            ((2, 32, 8, LANES), F32),
            ((2, 32, 8, LANES), F32),
            ((total, LANES), F32),
            ((3, WINDOW + 2 * MARGIN, LANES), F32),
            ((3, WINDOW + 2 * MARGIN, LANES), F32),
        ],
        bounds=True,
    )(lengths, n_mlp, up_own, table, stats, *cot, merge_weight, down_weight, attn)
    mixed_own = lax.all_to_all(mixed, "tm", 0, 0, tiled=True)

    def own_head(refs, buffer):
        at = pl.ds(pl.multiple_of(lax.axis_index("tm") * HEAD, HEAD), HEAD)
        return [(refs[0].at[at], buffer.at[pl.ds(0, HEAD)])]

    branch, from_attn, *head_packs, head_lines = kernel_call(
        attend_back_kernel,
        [
            ((total, D), BF16, 1),
            ((total, D), BF16, 1),
            *([((4 * HEAD + 8 * share, LANES), BF16, 1)] * quarters),
            ((8, D), F32),
        ],
        [
            blocks_part(),
            rows_part(0, D),
            Part((LANES, D), own_head),
            whole,
            late,
            late,
            late,
            "v",
            "v",
            late,
            Part((total, LANES), lambda refs, buffer: [(refs[0].at[:, pl.ds(0, LANES)], buffer)], late=True),
            late,
            late,
            late,
            late,
            "v",
            late,
        ],
        [
            ((total, LANES), BF16),
            ((total, total), BF16),
            ((total, D), BF16),
            ((total, 3 * LANES), BF16),
            ((4 * HEAD, D), F32),
        ],
    )(
        *cot,
        merge_weight,
        out_weight,
        attn,
        value,
        prob,
        key,
        coarse_table,
        fine_table,
        pos_own,
        query,
        n_attn,
        q_position,
        qkv_own,
        hat,
        ln_attn_gain,
        early_pack,
    )
    head_parts = over_streams(head_packs)
    mixed_own, _ = lax.optimization_barrier((mixed_own, head_lines))
    out_rows, joined = kernel_call(
        output_kernel,
        [((own, D), BF16), ((count, 256, own), BF16)],
        "vvvvvvv",
        megas=24,
    )(own_frames, mixed_own, out_weight, down_weight, down_bias, merge_weight, merge_bias)
    joined_all = lax.all_to_all(joined, "tm", 0, 0, tiled=True)
    gate_pre, _ = lax.optimization_barrier((gate_pre, joined))
    late_rows = 5 * share + 16 + 3 * D // count
    same, apart, late_pack = kernel_call(
        mlp_second_kernel,
        [((count // 2, own, D), BF16, 1)] * 2 + [((quarters, late_rows, LANES), BF16, 1)],
        [
            Part(
                (count, 2 * total // BLOCK, 2 * LANES),
                lambda refs, buffer: [(refs[0].at[:, pl.ds(own, 2 * total // BLOCK)], buffer)],
            ),
            *([whole] * 4),
            late,
            late,
            "v",
            late,
            late,
            *"vvv",
            late,
            late,
            blocks_part(late=True),
        ],
        [
            ((total, 3 * LANES), BF16),
            ((total, LANES), F32),
            ((2 * LANES, D), F32),
            ((16, D), F32),
            ((channels, LANES), F32),
            ((2 * D // count, D), F32),
            ((D // count, D), F32),
        ],
    )(
        mixed_own,
        gate_pre,
        grad_y,
        slope,
        gate_hat,
        up_own,
        hat,
        ln_mlp_gain,
        from_attn,
        n_mlp,
        vectors,
        first_lines,
        head_lines,
        joined_all,
        branch,
        *cot,
    )
    late_moved = lax.all_to_all(late_pack, "stream", 0, 0, tiled=True)
    apart, head_parts = lax.optimization_barrier((apart, head_parts))
    sibling = moved(apart, "tm", 1)
    (early_part,) = kernel_call(add_kernel, [((4 * HEAD + 8 * share, LANES), BF16)], quarters * "v", megas=24)(
        *head_parts
    )
    early_near = near_blocks(early_part)
    pairs = kernel_call(pair_kernel, [((own, D), BF16)] * (count // 2), "vv", megas=24)(same, sibling)
    sums = [pairs[0]] + [moved(pairs[slot], "tm", 2 * slot) for slot in range(1, count // 2)]
    late_moved, early_near, sums = lax.optimization_barrier((late_moved, early_near, sums))
    (late_part,) = kernel_call(add_streams_kernel, [((late_rows, LANES), BF16)], "v", megas=24)(late_moved)
    late_near = near_blocks(late_part)
    early_all = far_stack(early_near)
    (grad_frames,) = kernel_call(frames_kernel, [((own, D), F32)], (2 + count // 2) * "v", megas=24)(
        own_frames, own_cotangent, *sums
    )
    grad_qkv, grad_pos, grad_down, half_up = kernel_call(
        early_kernel,
        [
            ((quarter, 3 * D), F32),
            ((quarter, D), F32),
            ((HALF // quarters, D), F32),
            ((quarter, 2 * HALF), F32, 1, (quarter, HALF), lambda ref: ref.at[:, pl.ds(0, HALF)]),
        ],
        "vv",
        [((count, 4 * HEAD + 8 * share, LANES), BF16)],
        megas=24,
    )(*early_all)
    late_near, grad_frames, grad_pos = lax.optimization_barrier((late_near, grad_frames, grad_pos))
    late_parts = far_stack(late_near)
    late = kernel_call(
        late_kernel,
        [((quarter,), F32)] * 6
        + [
            ((quarter, D), F32),
            ((quarter, 2 * HALF), F32, 1, (quarter, HALF), lambda ref: ref.at[:, pl.ds(HALF, HALF)]),
            ((2 * HALF // quarters,), F32),
            ((HALF // quarters,), F32),
            ((HALF // quarters,), F32),
            ((KERNEL, HALF // quarters), F32),
            ((HALF // quarters,), F32),
            ((quarter,), F32),
            ((2 * D // quarters, D), F32),
            ((quarter,), F32),
        ],
        "kvv",
        [((count,) + late_part.shape, BF16)],
        megas=24,
        aliases={0: 7},
    )(half_up, *late_parts)
    return (
        out_rows[None],
        grad_frames[None],
        *late[:4],
        grad_qkv,
        *late[4:6],
        grad_pos,
        *late[6:13],
        grad_down,
        *late[13:],
    )


def per_device(*operands):
    fits = (
        lax.axis_size("tm") == HEADS
        and lax.axis_size("stream") * LANES == D
        and operands[0].shape[1] == BLOCK
    )
    return head_device(*operands) if fits else frame_device(*operands)


def solution(mesh):
    return jax.shard_map(
        per_device,
        mesh=mesh,
        in_specs=(
            P("stream", "tm", None),
            P("stream", None),
            P("stream", "tm", None),
            P(),
            P(),
            P(),
            P(),
            P(),
            P(),
            P(),
            P(),
            P(),
            P(),
            P(),
            P(),
            P(),
            P(),
            P(),
            P(),
            P(),
            P(),
            P(),
        ),
        out_specs=(
            P("stream", "tm", None),
            P("stream", "tm", None),
            P("stream"),
            P("stream"),
            P("stream"),
            P("stream"),
            P("stream", None),
            P("stream"),
            P("stream"),
            P("stream", None),
            P("stream", None),
            P("stream", None),
            P("stream"),
            P("stream"),
            P("stream"),
            P(None, "stream"),
            P("stream"),
            P("stream", None),
            P("stream"),
            P("stream", None),
            P("stream"),
        ),
        check_vma=False,
    )
```

```python
import math

import jax
import jax.numpy as jnp
from jax import lax
from jax.experimental import pallas as pl
from jax.experimental.pallas import tpu as pltpu
from jax.sharding import PartitionSpec as P

D = 512
HEADS = 8
HEAD = 64
KERNEL = 31
ITEMS = 5
HALF = 1536


EPS = 1e-05
MASKED = -1e30


def extended(block, sides, width):
    for axis, dim in sides:
        count = lax.axis_size(axis)
        forward = [(i, i + 1) for i in range(count - 1)]
        backward = [(target, source) for source, target in forward]
        low = lax.ppermute(
            lax.slice_in_dim(block, block.shape[dim] - width, None, axis=dim), axis, forward
        )
        high = lax.ppermute(lax.slice_in_dim(block, 0, width, axis=dim), axis, backward)
        block = jnp.concatenate([low, block, high], axis=dim)
    return block


def norm_rows(inputs, scale_row, shift_row):
    row_mean = jnp.mean(inputs, axis=-1, keepdims=True)
    centred = inputs - row_mean
    spread = jnp.mean(centred * centred, axis=-1, keepdims=True)
    return centred * lax.rsqrt(spread + EPS) * scale_row + shift_row


def gelu_exact(inputs):
    return jax.nn.gelu(inputs, approximate=False)


def frame_info(lengths, offset, extent):
    item_ends = jnp.cumsum(lengths)
    first_table = jnp.concatenate([item_ends - lengths, item_ends[-1:]])
    frame_index = offset + jnp.arange(extent, dtype=jnp.int32)
    item_of = jnp.sum((frame_index[:, None] >= item_ends[None, :]).astype(jnp.int32), axis=1)
    labels = jnp.arange(ITEMS + 1, dtype=jnp.int32)
    first_frame = jnp.sum(
        jnp.where(item_of[:, None] == labels[None, :], first_table[None, :], 0), axis=1
    )
    return (frame_index, item_of, frame_index - first_frame)


def angles(place_in):
    frequency = jnp.exp(jnp.arange(D // 2, dtype=jnp.float32) * (-2.0 * math.log(10000.0) / D))
    phase_angle = place_in.astype(jnp.float32)[:, None] * frequency[None, :]
    return (jnp.sin(phase_angle), jnp.cos(phase_angle))


def rel_query(projected, sine_rows, cosine_rows):
    half_size = projected.shape[-1] // 2
    first_half = projected[..., :half_size]
    second_half = projected[..., half_size:]
    sine_wide = sine_rows[:, None, :]
    cosine_wide = cosine_rows[:, None, :]
    return jnp.concatenate(
        [
            first_half * sine_wide + second_half * cosine_wide,
            second_half * sine_wide - first_half * cosine_wide,
        ],
        axis=-1,
    )


def step_size(extent):
    return math.gcd(extent, 512)


def score_block(q_content, q_rel, query_item, query_frame, key_block, key_start, lengths):
    extent = key_block.shape[0]
    key_frame, key_item, key_place = frame_info(lengths, key_start, extent)
    sine_rows, cosine_rows = angles(key_place)
    k_rel = jnp.concatenate([cosine_rows, sine_rows], axis=1).astype(jnp.bfloat16)
    raw_scores = jnp.einsum(
        "qhe,khe->hqk",
        q_content,
        key_block.reshape(extent, HEADS, HEAD),
        preferred_element_type=jnp.float32,
    )
    raw_scores = raw_scores + jnp.einsum(
        "qhc,kc->hqk", q_rel, k_rel, preferred_element_type=jnp.float32
    )
    allowed = (query_item[:, None] == key_item[None, :]) & (
        (query_item[:, None] < ITEMS) | (query_frame[:, None] == key_frame[None, :])
    )
    return (raw_scores, allowed, k_rel)


def block_grads(
    q_content,
    q_rel,
    query_item,
    query_frame,
    grad_out,
    log_total,
    delta_rows,
    key_block,
    value_block,
    key_start,
    lengths,
):
    extent = key_block.shape[0]
    raw_scores, allowed, k_rel = score_block(
        q_content, q_rel, query_item, query_frame, key_block, key_start, lengths
    )
    prob_rows = jnp.where(allowed[None], jnp.exp(raw_scores * 0.125 - log_total[:, :, None]), 0.0)
    grad_prob = jnp.einsum(
        "qhe,khe->hqk",
        grad_out,
        value_block.reshape(extent, HEADS, HEAD),
        preferred_element_type=jnp.float32,
    )
    grad_raw = (prob_rows * (grad_prob - delta_rows[:, :, None]) * 0.125).astype(jnp.bfloat16)
    return (prob_rows.astype(jnp.bfloat16), grad_raw, k_rel)


def frame_device(
    frames,
    lengths,
    cotangent,
    ln_attn_gain,
    ln_attn_bias,
    ln_mlp_gain,
    ln_mlp_bias,
    qkv_weight,
    content_bias,
    position_bias,
    pos_weight,
    out_weight,
    up_weight,
    up_bias,
    gate_norm_gain,
    gate_norm_bias,
    conv_kernel,
    conv_bias,
    down_weight,
    down_bias,
    merge_weight,
    merge_bias,
):
    row_count = frames.shape[1]
    cycle_size = lax.axis_size("tm")
    offset = lax.axis_index("tm") * row_count
    stream_lengths = lengths[0]
    inputs = frames[0].astype(jnp.float32)
    frame_index, item_of, place_in = frame_info(stream_lengths, offset, row_count)
    sine_rows, cosine_rows = angles(place_in)
    attn_norm, attn_pull = jax.vjp(
        norm_rows, inputs, ln_attn_gain.astype(jnp.float32), ln_attn_bias.astype(jnp.float32)
    )
    mlp_norm, mlp_pull = jax.vjp(
        norm_rows, inputs, ln_mlp_gain.astype(jnp.float32), ln_mlp_bias.astype(jnp.float32)
    )
    attn_norm_low = attn_norm.astype(jnp.bfloat16)
    mlp_norm_low = mlp_norm.astype(jnp.bfloat16)
    qkv_rows = jnp.dot(attn_norm_low, qkv_weight, preferred_element_type=jnp.float32)
    query_rows = qkv_rows[:, :D]
    key_rows = qkv_rows[:, D : 2 * D].astype(jnp.bfloat16)
    value_rows = qkv_rows[:, 2 * D :].astype(jnp.bfloat16)
    q_content = (query_rows + content_bias.astype(jnp.float32)).astype(jnp.bfloat16)
    q_position = (query_rows + position_bias.astype(jnp.float32)).astype(jnp.bfloat16)
    content_heads = q_content.reshape(row_count, HEADS, HEAD)
    position_heads = q_position.reshape(row_count, HEADS, HEAD)
    pos_heads = pos_weight.reshape(D, HEADS, HEAD)
    projected = jnp.einsum(
        "the,che->thc", position_heads, pos_heads, preferred_element_type=jnp.float32
    )
    q_rel = rel_query(projected, sine_rows, cosine_rows).astype(jnp.bfloat16)
    start_state = (
        jnp.full((HEADS, row_count), MASKED, jnp.float32),
        jnp.zeros((HEADS, row_count), jnp.float32),
        jnp.zeros((HEADS, row_count, HEAD), jnp.float32),
    )
    fold_state = start_state
    key_piece = lax.all_gather(key_rows, "tm", axis=0, tiled=True)
    value_piece = lax.all_gather(value_rows, "tm", axis=0, tiled=True)
    extent = key_piece.shape[0]
    step_rows = step_size(extent)

    def forward_one_step(inner_state, step_index):
        row_top, row_total, row_acc = inner_state
        key_block = lax.dynamic_slice_in_dim(key_piece, step_index * step_rows, step_rows, 0)
        value_block = lax.dynamic_slice_in_dim(value_piece, step_index * step_rows, step_rows, 0)
        raw_scores, allowed, k_rel = score_block(
            content_heads,
            q_rel,
            item_of,
            frame_index,
            key_block,
            step_index * step_rows,
            stream_lengths,
        )
        scaled = jnp.where(allowed[None], raw_scores * 0.125, MASKED)
        new_top = jnp.maximum(row_top, jnp.max(scaled, axis=2))
        weight = jnp.where(allowed[None], jnp.exp(scaled - new_top[:, :, None]), 0.0)
        factor = jnp.exp(row_top - new_top)
        row_total = row_total * factor + jnp.sum(weight, axis=2)
        row_acc = row_acc * factor[:, :, None] + jnp.einsum(
            "hqk,khe->hqe",
            weight.astype(jnp.bfloat16),
            value_block.reshape(step_rows, HEADS, HEAD),
            preferred_element_type=jnp.float32,
        )
        return ((new_top, row_total, row_acc), None)

    fold_state, unused = lax.scan(
        forward_one_step, fold_state, jnp.arange(extent // step_rows, dtype=jnp.int32)
    )
    row_top, row_total, row_acc = fold_state
    attn_heads = row_acc / row_total[:, :, None]
    log_total = row_top + jnp.log(row_total)
    attn_low = jnp.transpose(attn_heads, (1, 0, 2)).reshape(row_count, D).astype(jnp.bfloat16)
    branch_attn = jnp.dot(attn_low, out_weight, preferred_element_type=jnp.float32).astype(
        jnp.bfloat16
    )
    hidden_pre = jnp.dot(
        mlp_norm_low, up_weight, preferred_element_type=jnp.float32
    ) + up_bias.astype(jnp.float32)
    hidden, gelu_pull = jax.vjp(gelu_exact, hidden_pre)
    gate_half = hidden[:, :HALF]
    conv_norm, conv_pull = jax.vjp(
        norm_rows,
        hidden[:, HALF:],
        gate_norm_gain.astype(jnp.float32),
        gate_norm_bias.astype(jnp.float32),
    )
    conv_in = conv_norm.astype(jnp.bfloat16)
    half_width = KERNEL // 2
    conv_wide = extended(conv_in, (("tm", 0),), half_width)
    wide_frame, wide_item, wide_place = frame_info(
        stream_lengths, offset - half_width, row_count + 2 * half_width
    )
    kernel_rows = conv_kernel.astype(jnp.float32)
    conv_out = conv_bias.astype(jnp.float32) + jnp.zeros_like(gate_half)
    for tap_index in range(KERNEL):
        same_item = (wide_item[tap_index : tap_index + row_count] == item_of)[:, None]
        conv_out = (
            conv_out
            + jnp.where(
                same_item, conv_wide[tap_index : tap_index + row_count].astype(jnp.float32), 0.0
            )
            * kernel_rows[tap_index]
        )
    gated_low = (gate_half * conv_out).astype(jnp.bfloat16)
    branch_mlp = (
        jnp.dot(gated_low, down_weight, preferred_element_type=jnp.float32)
        + down_bias.astype(jnp.float32)
    ).astype(jnp.bfloat16)
    joined = jnp.concatenate([branch_attn, branch_mlp], axis=1)
    result = (
        inputs
        + jnp.dot(joined, merge_weight, preferred_element_type=jnp.float32)
        + merge_bias.astype(jnp.float32)
    )
    out_rows = result.astype(jnp.bfloat16)[None]
    grad_low = cotangent[0]
    grad_rows = grad_low.astype(jnp.float32)
    grad_merge_bias = jnp.sum(grad_rows, axis=0)
    grad_merge_weight = jnp.einsum(
        "tc,td->cd", joined, grad_low, preferred_element_type=jnp.float32
    )
    grad_joined = jnp.einsum(
        "td,cd->tc", grad_low, merge_weight, preferred_element_type=jnp.float32
    )
    grad_attn_branch = grad_joined[:, :D].astype(jnp.bfloat16)
    grad_mlp_branch = grad_joined[:, D:].astype(jnp.bfloat16)
    grad_down_weight = jnp.einsum(
        "tc,td->cd", gated_low, grad_mlp_branch, preferred_element_type=jnp.float32
    )
    grad_down_bias = jnp.sum(grad_mlp_branch.astype(jnp.float32), axis=0)
    grad_gated = jnp.einsum(
        "td,cd->tc", grad_mlp_branch, down_weight, preferred_element_type=jnp.float32
    )
    grad_gate_half = grad_gated * conv_out
    grad_conv_out = (grad_gated * gate_half).astype(jnp.bfloat16)
    grad_conv_rows = grad_conv_out.astype(jnp.float32)
    grad_conv_bias = jnp.sum(grad_conv_rows, axis=0)
    grad_wide = extended(grad_conv_out, (("tm", 0),), half_width)
    kernel_list = []
    grad_conv_in = jnp.zeros_like(grad_conv_rows)
    for tap_index in range(KERNEL):
        same_item = (wide_item[tap_index : tap_index + row_count] == item_of)[:, None]
        kernel_list.append(
            jnp.sum(
                jnp.where(
                    same_item, conv_wide[tap_index : tap_index + row_count].astype(jnp.float32), 0.0
                )
                * grad_conv_rows,
                axis=0,
            )
        )
        back_start = 2 * half_width - tap_index
        back_item = (wide_item[back_start : back_start + row_count] == item_of)[:, None]
        grad_conv_in = (
            grad_conv_in
            + jnp.where(
                back_item, grad_wide[back_start : back_start + row_count].astype(jnp.float32), 0.0
            )
            * kernel_rows[tap_index]
        )
    grad_conv_kernel = jnp.stack(kernel_list)
    grad_second, grad_gate_norm_gain, grad_gate_norm_bias = conv_pull(grad_conv_in)
    (grad_pre_rows,) = gelu_pull(jnp.concatenate([grad_gate_half, grad_second], axis=1))
    grad_pre = grad_pre_rows.astype(jnp.bfloat16)
    grad_up_bias = jnp.sum(grad_pre.astype(jnp.float32), axis=0)
    grad_up_weight = jnp.einsum(
        "tc,tf->cf", mlp_norm_low, grad_pre, preferred_element_type=jnp.float32
    )
    grad_mlp_norm = jnp.einsum("tf,cf->tc", grad_pre, up_weight, preferred_element_type=jnp.float32)
    grad_out_weight = jnp.einsum(
        "tc,td->cd", attn_low, grad_attn_branch, preferred_element_type=jnp.float32
    )
    grad_attn_low = jnp.einsum(
        "td,cd->tc", grad_attn_branch, out_weight, preferred_element_type=jnp.float32
    ).astype(jnp.bfloat16)
    grad_out_heads = grad_attn_low.reshape(row_count, HEADS, HEAD)
    delta_rows = jnp.sum(
        jnp.transpose(grad_out_heads.astype(jnp.float32), (1, 0, 2)) * attn_heads, axis=2
    )
    total_frames = row_count * cycle_size
    back_start_state = (
        jnp.zeros((row_count, HEADS, HEAD), jnp.float32),
        jnp.zeros((row_count, HEADS, D), jnp.float32),
        jnp.zeros((total_frames, D), jnp.float32),
        jnp.zeros((total_frames, D), jnp.float32),
    )
    back_key_piece = lax.all_gather(key_rows, "tm", axis=0, tiled=True)
    back_value_piece = lax.all_gather(value_rows, "tm", axis=0, tiled=True)
    extent = back_key_piece.shape[0]
    back_step_rows = step_size(extent)

    def back_one_step(inner_state, step_index):
        grad_content, grad_rel = inner_state
        key_block = lax.dynamic_slice_in_dim(
            back_key_piece, step_index * back_step_rows, back_step_rows, 0
        )
        value_block = lax.dynamic_slice_in_dim(
            back_value_piece, step_index * back_step_rows, back_step_rows, 0
        )
        prob_low, grad_raw, k_rel = block_grads(
            content_heads,
            q_rel,
            item_of,
            frame_index,
            grad_out_heads,
            log_total,
            delta_rows,
            key_block,
            value_block,
            step_index * back_step_rows,
            stream_lengths,
        )
        grad_content = grad_content + jnp.einsum(
            "hqk,khe->qhe",
            grad_raw,
            key_block.reshape(back_step_rows, HEADS, HEAD),
            preferred_element_type=jnp.float32,
        )
        grad_rel = grad_rel + jnp.einsum(
            "hqk,kc->qhc", grad_raw, k_rel, preferred_element_type=jnp.float32
        )
        key_part = jnp.einsum(
            "hqk,qhe->khe", grad_raw, content_heads, preferred_element_type=jnp.float32
        ).reshape(back_step_rows, D)
        value_part = jnp.einsum(
            "hqk,qhe->khe", prob_low, grad_out_heads, preferred_element_type=jnp.float32
        ).reshape(back_step_rows, D)
        return ((grad_content, grad_rel), (key_part, value_part))

    inner_state, block_parts = lax.scan(
        back_one_step,
        (back_start_state[0], back_start_state[1]),
        jnp.arange(extent // back_step_rows, dtype=jnp.int32),
    )
    key_all = block_parts[0].reshape(extent, D)
    value_all = block_parts[1].reshape(extent, D)
    grad_content, grad_rel, key_all, value_all = (
        inner_state[0],
        inner_state[1],
        key_all,
        value_all,
    )
    grad_keys, grad_values = (
        lax.psum_scatter(key_all, "tm", scatter_dimension=0, tiled=True),
        lax.psum_scatter(value_all, "tm", scatter_dimension=0, tiled=True),
    )
    half_size = D // 2
    rel_first = grad_rel[..., :half_size]
    rel_second = grad_rel[..., half_size:]
    sine_wide = sine_rows[:, None, :]
    cosine_wide = cosine_rows[:, None, :]
    grad_projected = jnp.concatenate(
        [
            rel_first * sine_wide - rel_second * cosine_wide,
            rel_first * cosine_wide + rel_second * sine_wide,
        ],
        axis=-1,
    ).astype(jnp.bfloat16)
    grad_pos_weight = jnp.einsum(
        "thc,the->che", grad_projected, position_heads, preferred_element_type=jnp.float32
    ).reshape(D, D)
    grad_q_position = jnp.einsum(
        "thc,che->the", grad_projected, pos_heads, preferred_element_type=jnp.float32
    )
    grad_content_bias = jnp.sum(grad_content, axis=0).reshape(D)
    grad_position_bias = jnp.sum(grad_q_position, axis=0).reshape(D)
    grad_query = (grad_content + grad_q_position).reshape(row_count, D).astype(jnp.bfloat16)
    grad_qkv = jnp.concatenate(
        [grad_query, grad_keys.astype(jnp.bfloat16), grad_values.astype(jnp.bfloat16)], axis=1
    )
    grad_qkv_weight = jnp.einsum(
        "tc,tf->cf", attn_norm_low, grad_qkv, preferred_element_type=jnp.float32
    )
    grad_attn_norm = jnp.einsum(
        "tf,cf->tc", grad_qkv, qkv_weight, preferred_element_type=jnp.float32
    )
    grad_from_attn, grad_ln_attn_gain, grad_ln_attn_bias = attn_pull(grad_attn_norm)
    grad_from_mlp, grad_ln_mlp_gain, grad_ln_mlp_bias = mlp_pull(grad_mlp_norm)
    grad_inputs = grad_rows + grad_from_attn + grad_from_mlp
    weight_grads = (
        grad_ln_attn_gain,
        grad_ln_attn_bias,
        grad_ln_mlp_gain,
        grad_ln_mlp_bias,
        grad_qkv_weight,
        grad_content_bias,
        grad_position_bias,
        grad_pos_weight,
        grad_out_weight,
        grad_up_weight,
        grad_up_bias,
        grad_gate_norm_gain,
        grad_gate_norm_bias,
        grad_conv_kernel,
        grad_conv_bias,
        grad_down_weight,
        grad_down_bias,
        grad_merge_weight,
        grad_merge_bias,
    )
    summed = lax.psum(
        (
            weight_grads[0],
            weight_grads[1],
            weight_grads[2],
            weight_grads[3],
            weight_grads[4],
            weight_grads[5],
            weight_grads[6],
            weight_grads[7],
            weight_grads[8],
            weight_grads[9],
            weight_grads[10],
            weight_grads[11],
            weight_grads[12],
            weight_grads[13],
            weight_grads[14],
            weight_grads[15],
            weight_grads[16],
            weight_grads[17],
            weight_grads[18],
        ),
        "tm",
    )
    shares = (
        lax.psum_scatter(
            summed[0].astype(jnp.bfloat16), "stream", scatter_dimension=0, tiled=True
        ).astype(jnp.float32),
        lax.psum_scatter(
            summed[1].astype(jnp.bfloat16), "stream", scatter_dimension=0, tiled=True
        ).astype(jnp.float32),
        lax.psum_scatter(
            summed[2].astype(jnp.bfloat16), "stream", scatter_dimension=0, tiled=True
        ).astype(jnp.float32),
        lax.psum_scatter(
            summed[3].astype(jnp.bfloat16), "stream", scatter_dimension=0, tiled=True
        ).astype(jnp.float32),
        lax.psum_scatter(
            summed[4].astype(jnp.bfloat16), "stream", scatter_dimension=0, tiled=True
        ).astype(jnp.float32),
        lax.psum_scatter(
            summed[5].astype(jnp.bfloat16), "stream", scatter_dimension=0, tiled=True
        ).astype(jnp.float32),
        lax.psum_scatter(
            summed[6].astype(jnp.bfloat16), "stream", scatter_dimension=0, tiled=True
        ).astype(jnp.float32),
        lax.psum_scatter(
            summed[7].astype(jnp.bfloat16), "stream", scatter_dimension=0, tiled=True
        ).astype(jnp.float32),
        lax.psum_scatter(
            summed[8].astype(jnp.bfloat16), "stream", scatter_dimension=0, tiled=True
        ).astype(jnp.float32),
        lax.psum_scatter(
            summed[9].astype(jnp.bfloat16), "stream", scatter_dimension=0, tiled=True
        ).astype(jnp.float32),
        lax.psum_scatter(
            summed[10].astype(jnp.bfloat16), "stream", scatter_dimension=0, tiled=True
        ).astype(jnp.float32),
        lax.psum_scatter(
            summed[11].astype(jnp.bfloat16), "stream", scatter_dimension=0, tiled=True
        ).astype(jnp.float32),
        lax.psum_scatter(
            summed[12].astype(jnp.bfloat16), "stream", scatter_dimension=0, tiled=True
        ).astype(jnp.float32),
        lax.psum_scatter(
            summed[13].astype(jnp.bfloat16), "stream", scatter_dimension=1, tiled=True
        ).astype(jnp.float32),
        lax.psum_scatter(
            summed[14].astype(jnp.bfloat16), "stream", scatter_dimension=0, tiled=True
        ).astype(jnp.float32),
        lax.psum_scatter(
            summed[15].astype(jnp.bfloat16), "stream", scatter_dimension=0, tiled=True
        ).astype(jnp.float32),
        lax.psum_scatter(
            summed[16].astype(jnp.bfloat16), "stream", scatter_dimension=0, tiled=True
        ).astype(jnp.float32),
        lax.psum_scatter(
            summed[17].astype(jnp.bfloat16), "stream", scatter_dimension=0, tiled=True
        ).astype(jnp.float32),
        lax.psum_scatter(
            summed[18].astype(jnp.bfloat16), "stream", scatter_dimension=0, tiled=True
        ).astype(jnp.float32),
    )
    return (out_rows, grad_inputs[None]) + tuple(shares)


LANES = 128
LOW = LANES // 2
BLOCK = 128
TALL = 256
WINDOW = 64
MARGIN = 16
BOUNDS = 16
MEGA = 1024 * 1024
F32 = jnp.float32
BF16 = jnp.bfloat16


def dot_nn(left, right):
    return jnp.dot(left, right, preferred_element_type=F32)


def dot_nt(left, right):
    return lax.dot_general(left, right, (((1,), (1,)), ((), ())), preferred_element_type=F32)


def dot_tn(left, right):
    return lax.dot_general(left, right, (((0,), (0,)), ((), ())), preferred_element_type=F32)


def rows_of(index, size, base=0):
    return pl.ds(pl.multiple_of(index * size, size) + base, size)


def line_of(ref):
    return ref[...].astype(F32).reshape(1, ref.shape[0])


def fold_rows(values):
    return jnp.sum(values.reshape(values.shape[0] // 8, 8, values.shape[1]), axis=0)


def one_row(values):
    return jnp.sum(values, axis=0, keepdims=True)


def turn(values):
    return pltpu.roll(values, LOW, 1)


def low_lanes(rows):
    return lax.broadcasted_iota(jnp.int32, (rows, LANES), 1) < LOW


def centre_rows(inputs):
    mean = jnp.mean(inputs, axis=-1, keepdims=True)
    centred = inputs - mean
    spread = jnp.mean(centred * centred, axis=-1, keepdims=True)
    return centred * lax.rsqrt(spread + EPS)


def gelu_parts(values):
    phi = 0.5 + 0.5 * lax.erf(values * math.sqrt(0.5))
    bell = jnp.exp(values * values * -0.5)
    return values * phi, phi + values * bell * (1.0 / math.sqrt(2.0 * math.pi))


class Part:
    def __init__(self, shape=None, pairs=None, refs=1, late=False):
        self.shape, self.pairs, self.refs, self.late = shape, pairs, refs, late

    def buffer(self, operand):
        return self.shape or operand.shape

    def copies(self, refs, buffer):
        return self.pairs(refs, buffer) if self.pairs else [(refs[0], buffer)]


def blocks_part(half, late=False):
    def pairs(refs, buffer):
        place = lax.axis_index("tm")
        return [
            (
                ref.at[:, pl.ds(half * D, D)],
                buffer.at[rows_of(lax.bitwise_xor(jnp.int32(apart), place), BLOCK)],
            )
            for apart, ref in enumerate(refs)
        ]

    return Part((HEADS * BLOCK, D), pairs, HEADS, late)


def rows_part(first, size, late=False):
    return Part((size, D), lambda refs, buffer: [(refs[0].at[pl.ds(first, size)], buffer)], late=late)


class Fetch:
    def __init__(self, pairs, buffer, sems, first):
        self.buffer, self.begun = buffer, False
        self.pending = [
            pltpu.make_async_copy(source, target, sems.at[first + index])
            for index, (source, target) in enumerate(pairs)
        ]

    def begin(self):
        if not self.begun:
            for copy in self.pending:
                copy.start()
        self.begun = True

    def __call__(self):
        self.begin()
        for copy in self.pending:
            copy.wait()
        self.pending = []
        return self.buffer


def begin(*fetches):
    for fetch in fetches:
        fetch.begin()


class Send:
    def __init__(self, buffer, target, sems):
        self.buffer, self.target, self.sems, self.copies = buffer, target, sems, []

    def go(self, *index):
        source, target = (self.buffer.at[index], self.target.at[index]) if index else (self.buffer, self.target)
        copy = pltpu.make_async_copy(source, target, self.sems[len(self.copies)])
        copy.start()
        self.copies.append(copy)

    def finish(self):
        if not self.copies:
            self.go()


SPACES = {"v": pltpu.VMEM, "s": pltpu.SMEM, "k": pl.ANY}


def kernel_call(body, out_shapes, plan, scratch=(), megas=58, bounds=False, aliases=None):
    def call(*operands):
        in_specs, buffers, at = [], [], 0
        for item in plan:
            if item == "f":
                in_specs.append(pl.BlockSpec(memory_space=pl.ANY))
                buffers.append(pltpu.VMEM(operands[at].shape, operands[at].dtype))
                at += 1
            elif isinstance(item, Part):
                in_specs += [pl.BlockSpec(memory_space=pl.ANY)] * item.refs
                buffers.append(pltpu.VMEM(item.buffer(operands[at]), operands[at].dtype))
                at += item.refs
            else:
                in_specs.append(pl.BlockSpec(memory_space=SPACES[item]))
                at += 1
        sent = [out for out in out_shapes if len(out) > 2]
        buffers += [pltpu.VMEM(out[3] if len(out) > 3 else out[0], out[1]) for out in sent]
        sem_count = 96
        extra = [pltpu.SMEM((BOUNDS,), jnp.int32)] if bounds else []

        def outer(*refs):
            inputs, rest = refs[: len(in_specs)], refs[len(in_specs) :]
            outputs, rest = rest[: len(out_shapes)], rest[len(out_shapes) :]
            held, rest = list(rest[: len(buffers)]), rest[len(buffers) :]
            sems, rest = rest[0], rest[1:]
            given, at, used = [], 0, 0
            for item in plan:
                if item == "f":
                    given.append(Fetch([(inputs[at], held[0])], held.pop(0), sems, used))
                    given[-1].begin()
                    used += 1
                    at += 1
                elif isinstance(item, Part):
                    buffer = held.pop(0)
                    pairs = item.copies(inputs[at : at + item.refs], buffer)
                    given.append(Fetch(pairs, buffer, sems, used))
                    if not item.late:
                        given[-1].begin()
                    used += len(pairs)
                    at += item.refs
                else:
                    given.append(inputs[at])
                    at += 1
            results = []
            for out, ref in zip(out_shapes, outputs):
                if len(out) > 2:
                    target = out[4](ref) if len(out) > 3 else ref
                    results.append(Send(held.pop(0), target, [sems.at[used + index] for index in range(4)]))
                    used += 4
                else:
                    results.append(ref)
            assert used <= sem_count
            given = [item() if kind == "f" else item for kind, item in zip(plan, given)]
            body(*given, *results, *rest)
            for item in given:
                if isinstance(item, Fetch):
                    item()
            sends = [item for item in results if isinstance(item, Send)]
            for item in sends:
                item.finish()
            for item in sends:
                for copy in item.copies:
                    copy.wait()

        return pl.pallas_call(
            outer,
            out_shape=[jax.ShapeDtypeStruct(out[0], out[1]) for out in out_shapes],
            in_specs=in_specs,
            out_specs=[pl.BlockSpec(memory_space=pl.ANY if len(out) > 2 else pltpu.VMEM) for out in out_shapes],
            scratch_shapes=buffers
            + [pltpu.SemaphoreType.DMA((sem_count,))]
            + [pltpu.VMEM(shape, kind) for shape, kind in scratch]
            + extra,
            input_output_aliases=aliases or {},
            compiler_params=pltpu.CompilerParams(vmem_limit_bytes=megas * MEGA),
            cost_estimate=pl.CostEstimate(flops=0, bytes_accessed=0, transcendentals=0),
        )(*operands)

    return call


def fill_bounds(lengths_ref, bounds_s, total):
    bounds_s[0] = jnp.int32(0)
    end = jnp.int32(0)
    for item in range(ITEMS):
        end = end + lengths_ref[0, item]
        bounds_s[item + 1] = end
    for item in range(ITEMS + 1, BOUNDS):
        bounds_s[item] = jnp.int32(total)


def select_kernel(
    up_ref,
    up_bias_ref,
    gain_ref,
    bias_ref,
    conv_bias_ref,
    taps_ref,
    qkv_ref,
    pos_ref,
    content_ref,
    position_ref,
    up_out,
    table_out,
    qkv_out,
    pos_out,
    bias_out,
):
    place = lax.axis_index("tm")
    quarters = lax.axis_size("stream")
    share = HALF // (quarters * lax.axis_size("tm"))
    lane = lax.broadcasted_iota(jnp.int32, (1, 2 * LANES), 1)
    channel = jnp.where(lane < LANES + LOW, lane, lane - LOW)
    group = jnp.zeros_like(channel)
    for quarter in range(1, quarters):
        group = group + (channel >= quarter * share).astype(jnp.int32)
    source = group * (HALF // quarters) + share * place + channel - group * share
    chosen = (lax.broadcasted_iota(jnp.int32, (HALF, 2 * LANES), 0) == source).astype(F32).astype(BF16)
    gate = dot_nn(up_ref[:, :HALF], chosen)
    conv = dot_nn(up_ref[:, HALF:], chosen)
    up_out[:, :LANES] = gate[:, :LANES].astype(BF16)
    up_out[:, LANES : 2 * LANES] = jnp.where(low_lanes(D), gate[:, LANES:], conv[:, LANES:]).astype(BF16)
    up_out[:, 2 * LANES :] = conv[:, :LANES].astype(BF16)
    up_bias = line_of(up_bias_ref)
    lines = jnp.concatenate(
        [
            up_bias[:, :HALF],
            up_bias[:, HALF:],
            line_of(gain_ref),
            line_of(bias_ref),
            line_of(conv_bias_ref),
            jnp.zeros((3, HALF), F32),
        ],
        axis=0,
    )
    lines = dot_nn(lines.astype(BF16), chosen)
    taps = dot_nn(taps_ref[...], chosen)
    for part in range(2):
        lanes = slice(part * LANES, (part + 1) * LANES)
        table_out[part, :8] = lines[:, lanes]
        table_out[part, 8 : 8 + KERNEL] = taps[:, lanes]
        table_out[part, 8 + KERNEL :] = jnp.zeros((1, LANES), F32)

    odd = lax.rem(place, 2) == 1

    def head_lanes(ref, base):
        at = pl.ds(pl.multiple_of(lax.div(place, 2) * LANES + base, LANES), LANES)
        values = ref[:, at].astype(F32)
        values = jnp.where(odd, turn(values), values)
        return jnp.where(low_lanes(values.shape[0]), values, 0.0)

    for part in range(3):
        qkv_out[:, part * LANES : (part + 1) * LANES] = head_lanes(qkv_ref, part * D).astype(BF16)
    pos_out[...] = head_lanes(pos_ref, 0).astype(BF16)
    bias_out[...] = jnp.zeros((8, LANES), F32)
    for line, ref in enumerate((content_ref, position_ref)):
        values = line_of(ref)
        picked = values[:, :LANES]
        for tile in range(1, D // LANES):
            picked = jnp.where(
                lax.div(place, 2) == tile, values[:, tile * LANES : (tile + 1) * LANES], picked
            )
        picked = jnp.where(odd, turn(picked), picked)
        bias_out[line : line + 1] = jnp.where(low_lanes(1), picked, 0.0)


def angle_rows(coarse_ref, fine_ref, block, rows):
    half = D // 2
    base = coarse_ref[pl.ds(block, 1)]
    base_sine, base_cosine = base[:, :half], base[:, half:]
    sine, cosine = fine_ref[rows, :half], fine_ref[rows, half:]
    return base_sine * cosine + base_cosine * sine, base_cosine * cosine - base_sine * sine


def item_codes(bounds_s, index):
    code = jnp.zeros_like(index)
    for item in range(1, ITEMS + 1):
        code = code + (index >= bounds_s[item]).astype(jnp.int32)
    return jnp.where(code < ITEMS, code, ITEMS + index)


def attend_kernel(
    lengths_ref,
    x_ref,
    attn_gain_ref,
    attn_bias_ref,
    mlp_gain_ref,
    mlp_bias_ref,
    qkv_ref,
    pos_ref,
    bias_ref,
    coarse_ref,
    fine_ref,
    up_ref,
    up_bias_ref,
    n_attn_out,
    n_mlp_out,
    hat_out,
    q_position_out,
    query_out,
    key_out,
    value_out,
    prob_out,
    attn_out,
    stats_out,
    bounds_s,
):
    frames = n_attn_out.buffer.shape[0]
    half = D // 2
    fill_bounds(lengths_ref, bounds_s, frames)
    attn_gain, attn_bias = line_of(attn_gain_ref), line_of(attn_bias_ref)
    mlp_gain, mlp_bias = line_of(mlp_gain_ref), line_of(mlp_bias_ref)
    content, position = bias_ref[0:1], bias_ref[1:2]
    x_ref = x_ref()
    begin(up_ref)

    @pl.loop(0, frames // TALL, unroll=4)
    def _(block):
        rows = rows_of(block, TALL)
        for part in range(TALL // 32):
            at = pl.ds(pl.multiple_of(block * TALL + part * 32, 32), 32)
            hat = centre_rows(x_ref[at].astype(F32))
            hat_out.buffer[at] = hat.astype(BF16)
            n_attn_out.buffer[at] = (hat * attn_gain + attn_bias).astype(BF16)
            n_mlp_out.buffer[at] = (hat * mlp_gain + mlp_bias).astype(BF16)
        parts = dot_nn(n_attn_out.buffer[rows], qkv_ref[...])
        query = parts[:, :LANES]
        query_out.buffer[rows, :LANES] = ((query + content).astype(BF16).astype(F32) * 0.125).astype(BF16)
        q_position = (query + position).astype(BF16)
        q_position_out.buffer[rows] = q_position
        key_out.buffer[rows, :LANES] = parts[:, LANES : 2 * LANES].astype(BF16)
        value_out.buffer[rows] = parts[:, 2 * LANES :].astype(BF16)
        projected = dot_nt(q_position, pos_ref[...])
        for part in range(TALL // 32):
            at = pl.ds(pl.multiple_of(block * TALL + part * 32, 32), 32)
            inner = part * 32 % BLOCK
            sine, cosine = angle_rows(
                coarse_ref, fine_ref, block * (TALL // BLOCK) + part * 32 // BLOCK, slice(inner, inner + 32)
            )
            first = projected[part * 32 : part * 32 + 32, :half]
            second = projected[part * 32 : part * 32 + 32, half:]
            query_out.buffer[at, LANES : LANES + half] = ((first * sine + second * cosine) * 0.125).astype(BF16)
            query_out.buffer[at, LANES + half :] = ((second * sine - first * cosine) * 0.125).astype(BF16)
            key_out.buffer[at, LANES : LANES + half] = cosine.astype(BF16)
            key_out.buffer[at, LANES + half :] = sine.astype(BF16)

    for out in (n_attn_out, n_mlp_out, hat_out, q_position_out, query_out, key_out, value_out):
        out.go()
    up_ref = up_ref()
    up_bias = line_of(up_bias_ref)[:, HALF:]
    lane = lax.broadcasted_iota(jnp.int32, (16, LANES), 1)

    @pl.loop(0, frames // TALL, unroll=2)
    def _(block):
        values = dot_nn(n_mlp_out.buffer[rows_of(block, TALL)], up_ref[...])
        for part in range(TALL // 16):
            pre = values[part * 16 : part * 16 + 16] + up_bias
            hidden = pre * (0.5 + 0.5 * lax.erf(pre * math.sqrt(0.5)))
            mean = jnp.mean(hidden, axis=-1, keepdims=True)
            centred = hidden - mean
            rate = lax.rsqrt(jnp.mean(centred * centred, axis=-1, keepdims=True) + EPS)
            at = pl.ds(pl.multiple_of(block * TALL + part * 16, 16), 16)
            stats_out.buffer[at] = jnp.where(lane == 0, mean, rate)

    stats_out.go()
    key_code = item_codes(bounds_s, lax.broadcasted_iota(jnp.int32, (1, frames), 1))

    low = low_lanes(32)
    for block in range(frames // TALL):
        rows = pl.ds(block * TALL, TALL)
        raw = dot_nt(query_out.buffer[rows], key_out.buffer[...])
        shares = []
        for part in range(TALL // 32):
            start = block * TALL + part * 32
            index = start + lax.broadcasted_iota(jnp.int32, (32, 1), 0)
            scaled = jnp.where(
                item_codes(bounds_s, index) == key_code, raw[part * 32 : part * 32 + 32], MASKED
            )
            weight = jnp.exp(scaled - jnp.max(scaled, axis=1, keepdims=True))
            prob_out.buffer[pl.ds(start, 32)] = weight.astype(BF16)
            shares.append(1.0 / jnp.sum(weight, axis=1, keepdims=True))
        prob_out.go(rows)
        attn = dot_nn(prob_out.buffer[rows], value_out.buffer[...])
        for part in range(TALL // 32):
            share = shares[part]
            attn_out.buffer[pl.ds(block * TALL + part * 32, 32)] = jnp.where(
                low, attn[part * 32 : part * 32 + 32] * share, share
            )


def fill_margins(wide_s, frames):
    edge = jnp.zeros((MARGIN, LANES), F32)
    wide_s[0, :MARGIN] = edge
    wide_s[0, MARGIN + frames : 2 * MARGIN + frames] = edge
    base = frames + 3 * MARGIN
    after = base + frames // 2
    low = low_lanes(MARGIN)
    wide_s[0, base - MARGIN : base] = jnp.where(low, 0.0, turn(wide_s[0, after - MARGIN : after]))
    wide_s[0, after : after + MARGIN] = jnp.where(low, turn(wide_s[0, base : base + MARGIN]), 0.0)
    wide_s[0, after + MARGIN :] = jnp.zeros((wide_s.shape[1] - after - MARGIN, LANES), F32)

    @pl.loop(0, (after + MARGIN) // WINDOW, unroll=5)
    def _(step):
        window = wide_s[0, pl.ds(pl.multiple_of(step * WINDOW, WINDOW), WINDOW + 8)]
        for shift in range(1, 8):
            wide_s[shift, pl.ds(pl.multiple_of(step * WINDOW, WINDOW), WINDOW)] = window[shift : shift + WINDOW]


def item_span(bounds_s, frame):
    begin, end = bounds_s[0], bounds_s[BOUNDS - 1]
    for item in range(1, ITEMS + 1):
        edge = bounds_s[item]
        begin = jnp.where(frame >= edge, edge, begin)
    for item in range(ITEMS, 0, -1):
        edge = bounds_s[item]
        end = jnp.where(frame < edge, edge, end)
    return begin, end


def is_whole(bounds_s, start):
    begin, end = item_span(bounds_s, start)
    reach = KERNEL // 2
    low = (begin == 0) | (begin <= start - reach)
    high = (end == bounds_s[BOUNDS - 1]) | (end >= start + WINDOW + reach)
    return low & high & (end >= start + WINDOW)


def tap_limits(bounds_s, start):
    frame = start + lax.broadcasted_iota(jnp.int32, (WINDOW, LANES), 0)
    begin, end = item_span(bounds_s, frame)
    return begin - frame, end - frame


def grouped(values):
    return values.reshape(WINDOW // 8, 8, LANES)


def triple_places(step, frames):
    half = frames // 2
    return (
        pl.multiple_of(step * WINDOW, 2 * MARGIN),
        pl.multiple_of(step * WINDOW + half, 2 * MARGIN),
        pl.multiple_of(step * WINDOW + frames + 2 * MARGIN, 2 * MARGIN),
    )


def over_windows(bounds_s, frames, body):
    half = frames // 2

    @pl.loop(0, half // WINDOW)
    def _(step):
        start = step * WINDOW
        whole = is_whole(bounds_s, start) & is_whole(bounds_s, start + half)

        @pl.when(whole)
        def _():
            body(step, None)

        @pl.when(jnp.logical_not(whole))
        def _():
            first, second = tap_limits(bounds_s, start), tap_limits(bounds_s, start + half)
            low = low_lanes(WINDOW)
            rest = [jnp.where(low, one, other) for one, other in zip(first, second)]
            body(step, (first, second, rest))


def tap_mask(tap, limits):
    shift = tap - KERNEL // 2
    return None if limits is None else (limits[0] <= shift) & (limits[1] > shift)


def tap_view(wide_s, base, tap, mask):
    at = pl.ds(pl.multiple_of(base + (tap + 1) // 8 * 8, 8), WINDOW)
    view = wide_s[(tap + 1) % 8, at]
    return grouped(view if mask is None else jnp.where(mask, view, 0.0))


def mlp_first_kernel(
    lengths_ref,
    n_ref,
    up_ref,
    table_ref,
    stats_ref,
    cot_ref,
    merge_ref,
    down_ref,
    attn_ref,
    mixed_out,
    gate_pre_out,
    grad_out,
    rate_out,
    hat_out,
    early_out,
    vectors_out,
    lines_out,
    hat_s,
    slope_s,
    gate_s,
    hidden_s,
    gate_slope_s,
    conv_s,
    grad_s,
    out_s,
    back_s,
    branch_s,
    mix_s,
    taps_s,
    turn_s,
    tap_sum_s,
    columns_s,
    bounds_s,
):
    frames = mix_s.shape[0]
    half = frames // 2
    blocks = frames // BLOCK
    quarters, early_rows, _ = early_out.buffer.shape
    share = early_rows // 8
    channels = quarters * share
    fill_bounds(lengths_ref, bounds_s, frames)
    for part in range(2):
        for tap in range(KERNEL):
            line = jnp.broadcast_to(table_ref[part, 8 + tap : 9 + tap], (8, LANES))
            taps_s[part, tap] = line
            turn_s[part, KERNEL - 1 - tap] = line
    tap_sum_s[...] = jnp.zeros(tap_sum_s.shape, F32)
    main, rest = table_ref[0, :8], table_ref[1, :8]
    mixed_bias = jnp.where(low_lanes(1), rest[0:1], rest[1:2])
    low = low_lanes(64)
    gate_pre_ref = gate_pre_out.buffer
    n_ref = n_ref()
    stats_ref = stats_ref()
    begin(cot_ref, merge_ref, down_ref, attn_ref)

    def stat_rows(rows):
        stats = stats_ref[rows]
        return stats[:, 0:1], stats[:, 1:2]

    def chunk(start, base=0):
        return pl.ds(pl.multiple_of(start, 64) + base, 64)

    def conv_part(hidden, mean, rate, lines, rows, to_rows):
        hat = (hidden - mean) * rate
        hat_s[rows] = hat
        hat_out.buffer[rows] = hat.astype(BF16)
        conv_s[0, to_rows] = (hat * lines[2:3] + lines[3:4]).astype(BF16).astype(F32)

    @pl.loop(0, half // TALL, unroll=2)
    def _(block):
        pre = [dot_nn(n_ref[rows_of(block, TALL, base)], up_ref[...]) for base in (0, half)]
        for part in range(TALL // 64):
            inner = slice(part * 64, part * 64 + 64)
            start = block * TALL + part * 64
            mixed = []
            for values, base in zip(pre, (0, half)):
                rows = chunk(start, base)
                gate, gate_slope = gelu_parts(values[inner, :LANES] + main[0:1])
                hidden_s[rows] = gate
                gate_slope_s[rows] = gate_slope
                hidden, slope = gelu_parts(values[inner, 2 * LANES :] + main[1:2])
                mean, rate = stat_rows(rows)
                slope_s[rows] = slope * rate
                conv_part(hidden, mean, rate, main, rows, chunk(start, base + MARGIN))
                mixed.append((*gelu_parts(values[inner, LANES : 2 * LANES] + mixed_bias), mean, rate))
            (low_hidden, low_slope, low_mean, low_rate), (high_hidden, high_slope, high_mean, high_rate) = mixed
            rows = chunk(start, frames)
            hidden_s[rows] = jnp.where(low, low_hidden, turn(high_hidden))
            gate_slope_s[rows] = jnp.where(low, low_slope, turn(high_slope))
            rate = jnp.where(low, low_rate, high_rate)
            slope_s[rows] = jnp.where(low, turn(low_slope), high_slope) * rate
            conv_part(
                jnp.where(low, turn(low_hidden), high_hidden),
                jnp.where(low, low_mean, high_mean),
                rate,
                rest,
                rows,
                chunk(start, frames + 3 * MARGIN),
            )

    hat_out.go()
    fill_margins(conv_s, frames)
    outs = (0, half, frames)

    def convolve(step, limits):
        for index, base in enumerate(triple_places(step, frames)):
            own = None if limits is None else limits[index]
            total = jnp.zeros((WINDOW // 8, 8, LANES), F32)
            for tap in range(KERNEL):
                view = tap_view(conv_s, base, tap, tap_mask(tap, own))
                total = total + view * taps_s[index // 2, tap][None]
            lines = rest if index == 2 else main
            out_s[rows_of(step, WINDOW, outs[index])] = total.reshape(WINDOW, LANES) + lines[4:5]

    over_windows(bounds_s, frames, convolve)
    cot_ref = cot_ref()
    merge_ref = merge_ref()
    down_ref = down_ref()
    attn_ref = attn_ref()
    down_ref[channels:] = jnp.zeros((2 * LANES - channels, D), BF16)
    zero = jnp.zeros((8, LANES), F32)

    def branch_part(grad_gated, rows, to_rows, sums):
        up_sum, conv_sum = sums
        gate, conv = hidden_s[rows], out_s[rows]
        gate_pre = (grad_gated * conv * gate_slope_s[rows]).astype(BF16)
        gate_pre_ref[rows] = gate_pre
        grad_conv = (grad_gated * gate).astype(BF16).astype(F32)
        grad_s[0, to_rows] = grad_conv
        gate_pre = gate_pre.astype(F32)
        return gate * conv, gate_pre, (up_sum + fold_rows(gate_pre), conv_sum + fold_rows(grad_conv))

    def branch_step(block, sums):
        main_sums, rest_sums = sums
        grads = []
        for base in (0, half):
            rows = rows_of(block, TALL, base)
            branch = dot_nt(cot_ref[rows], merge_ref[...]).astype(BF16)
            branch_s[rows] = branch
            grads.append(dot_nt(branch, down_ref[...]))
        for part in range(TALL // 64):
            inner = slice(part * 64, part * 64 + 64)
            start = block * TALL + part * 64
            for values, base in zip(grads, (0, half)):
                rows = chunk(start, base)
                gated, gate_pre, main_sums = branch_part(
                    values[inner, :LANES], rows, chunk(start, base + MARGIN), main_sums
                )
                mix_s[rows, :LANES] = gated.astype(BF16)
                gate_s[rows, :LANES] = gate_pre.astype(BF16)
            grad = jnp.where(low, grads[0][inner, LANES:], turn(grads[1][inner, LANES:]))
            gated, gate_pre, rest_sums = branch_part(
                grad, chunk(start, frames), chunk(start, frames + 3 * MARGIN), rest_sums
            )
            low_rows, high_rows = chunk(start), chunk(start, half)
            gate_s[low_rows, LANES:] = gate_pre.astype(BF16)
            gate_s[high_rows, LANES:] = turn(gate_pre).astype(BF16)
            mix_s[low_rows, LANES:] = jnp.where(low, gated, turn(attn_ref[low_rows])).astype(BF16)
            mix_s[high_rows, LANES:] = jnp.where(low, turn(gated), turn(attn_ref[high_rows])).astype(BF16)
        return main_sums, rest_sums

    (main_up, main_conv), (rest_up, rest_conv) = lax.fori_loop(
        0, half // TALL, branch_step, ((zero, zero), (zero, zero)), unroll=2
    )
    gate_pre_out.go()
    fill_margins(grad_s, frames)
    ones = jnp.ones((16, frames), BF16)
    lines_out[0:1] = dot_nn(ones, branch_s[...])[0:1]
    lines_out[1:2] = dot_nn(ones, cot_ref[...])[0:1]
    lines_out[2:8] = jnp.zeros((6, D), F32)
    grad_down = dot_tn(mix_s[...], branch_s[...])
    grad_gate = dot_tn(gate_s[...], n_ref[...])
    for quarter in range(quarters):
        for tile in range(4):
            early_out.buffer[quarter, tile * share : (tile + 1) * share] = grad_down[
                quarter * share : (quarter + 1) * share, tile * LANES : (tile + 1) * LANES
            ].astype(BF16)
        early_out.buffer[quarter, 4 * share :] = grad_gate[
            :channels, quarter * LANES : (quarter + 1) * LANES
        ].astype(BF16)
    early_out.go()
    for block in range(blocks):
        mixed_out.buffer[block, :BLOCK] = mix_s[block * BLOCK : (block + 1) * BLOCK]
    mixed_out.go(slice(None), pl.ds(0, BLOCK))

    def differentiate(step, limits):
        for index, base in enumerate(triple_places(step, frames)):
            own = None if limits is None else limits[index]
            total = jnp.zeros((WINDOW // 8, 8, LANES), F32)
            centre = grouped(grad_s[0, pl.ds(base + MARGIN, WINDOW)])
            for tap in range(KERNEL):
                mask = tap_mask(tap, own)
                total = total + tap_view(grad_s, base, tap, mask) * turn_s[index // 2, tap][None]
                tap_sum_s[index // 2, tap] += jnp.sum(tap_view(conv_s, base, tap, mask) * centre, axis=0)
            back_s[rows_of(step, WINDOW, outs[index])] = total.reshape(WINDOW, LANES)

    over_windows(bounds_s, frames, differentiate)
    lane = lax.broadcasted_iota(jnp.int32, (64, LANES), 1)

    def norm_part(rows, lines, sums):
        gain_sum, bias_sum = sums
        back, hat, slope = back_s[rows], hat_s[rows], slope_s[rows]
        grad = back * lines[2:3]
        grad_out.buffer[rows] = (grad * slope).astype(BF16)
        rate_out.buffer[rows] = slope.astype(BF16)
        along = back * hat
        return grad, along * lines[2:3], (gain_sum + fold_rows(along), bias_sum + fold_rows(back))

    def norm_step(block, sums):
        main_sums, rest_sums = sums
        for part in range(TALL // 64):
            start = block * TALL + part * 64
            pairs = []
            for base in (0, half):
                plain, along, main_sums = norm_part(chunk(start, base), main, main_sums)
                pairs.append([plain, along])
            plain, along, rest_sums = norm_part(chunk(start, frames), rest, rest_sums)
            for item, values in enumerate((plain, along)):
                pairs[0][item] = pairs[0][item] + jnp.where(low, values, 0.0)
                pairs[1][item] = pairs[1][item] + jnp.where(low, 0.0, values)
            for (plain, along), base in zip(pairs, (0, half)):
                columns_s[chunk(start, base)] = jnp.where(
                    lane == 0,
                    jnp.sum(plain, axis=-1, keepdims=True),
                    jnp.where(lane == 1, jnp.sum(along, axis=-1, keepdims=True), 0.0),
                )
        return main_sums, rest_sums

    (main_gain, main_bias), (rest_gain, rest_bias) = lax.fori_loop(
        0, half // TALL, norm_step, ((zero, zero), (zero, zero)), unroll=2
    )
    grad_out.go()
    rate_out.go()
    totals = jnp.concatenate(
        [jnp.transpose(columns_s[block * BLOCK : (block + 1) * BLOCK])[:2] for block in range(blocks)], axis=0
    )
    high = totals.astype(BF16)
    low_part = (totals - high.astype(F32)).astype(BF16)
    for block in range(blocks):
        mixed_out.buffer[block, BLOCK:, :LANES] = high
        mixed_out.buffer[block, BLOCK:, LANES:] = low_part
    mixed_out.go(slice(None), pl.ds(BLOCK, 2 * blocks))

    def vectors(part, lines):
        taps = jnp.sum(tap_sum_s[part], axis=1)[:KERNEL]
        stacked = jnp.concatenate([taps] + [one_row(line) for line in lines], axis=0)
        if part:
            stacked = stacked + turn(stacked)
        return jnp.transpose(
            jnp.concatenate([stacked, jnp.zeros((LANES - stacked.shape[0], LANES), F32)], axis=0)
        )

    vectors_out[:LANES] = vectors(0, (main_conv, main_gain, main_bias, main_up))
    vectors_out[LANES:] = vectors(1, (rest_conv, rest_gain, rest_bias, rest_up))[: channels - LANES]


def attend_back_kernel(
    cot_ref,
    merge_ref,
    head_ref,
    attn_ref,
    value_ref,
    prob_ref,
    key_ref,
    coarse_ref,
    fine_ref,
    pos_ref,
    query_ref,
    n_ref,
    q_position_ref,
    qkv_ref,
    hat_ref,
    gain_ref,
    early_ref,
    branch_out,
    total_out,
    pack_0,
    pack_1,
    pack_2,
    pack_3,
    lines_out,
    grad_s,
    raw_s,
    projected_s,
    parts_s,
    grads_s,
):
    place = lax.axis_index("tm")
    frames = raw_s.shape[0]
    blocks = frames // BLOCK
    half = D // 2
    zero = jnp.zeros((8, LANES), F32)
    cot_ref, merge_ref, head_ref, attn_ref = cot_ref(), merge_ref(), head_ref(), attn_ref()
    head_ref[HEAD:] = jnp.zeros((LANES - HEAD, D), BF16)
    begin(value_ref, prob_ref, key_ref, pos_ref)

    @pl.loop(0, frames // TALL, unroll=4)
    def _(block):
        rows = rows_of(block, TALL)
        branch = dot_nt(cot_ref[rows], merge_ref[...]).astype(BF16)
        branch_out.buffer[rows] = branch
        grad_s[rows] = (dot_nt(branch, head_ref[...]) * attn_ref[rows, HEAD : HEAD + 1]).astype(BF16)

    branch_out.go()
    value_ref, prob_ref = value_ref(), prob_ref()
    key_ref, pos_ref = key_ref(), pos_ref()
    begin(query_ref, n_ref, q_position_ref, qkv_ref, hat_ref, early_ref)

    def score_step(block, sums):
        content_sum, position_sum = sums
        rows = rows_of(block, TALL)
        grad = grad_s[rows]
        score = dot_nt(grad, value_ref[...])
        for part in range(TALL // 32):
            at = pl.ds(pl.multiple_of(block * TALL + part * 32, 32), 32)
            inner = slice(part * 32, part * 32 + 32)
            delta = jnp.sum(grad[inner].astype(F32) * attn_ref[at], axis=1, keepdims=True)
            raw_s[at] = (prob_ref[at].astype(F32) * (score[inner] - delta)).astype(BF16)
        query = dot_nn(raw_s[rows], key_ref[...]) * 0.125
        for part in range(TALL // 32):
            at = pl.ds(pl.multiple_of(block * TALL + part * 32, 32), 32)
            inner = part * 32 % BLOCK
            sine, cosine = angle_rows(
                coarse_ref, fine_ref, block * (TALL // BLOCK) + part * 32 // BLOCK, slice(inner, inner + 32)
            )
            inner = slice(part * 32, part * 32 + 32)
            first, second = query[inner, LANES : LANES + half], query[inner, LANES + half :]
            projected_s[at, :half] = (first * sine - second * cosine).astype(BF16)
            projected_s[at, half:] = (first * cosine + second * sine).astype(BF16)
        position = dot_nn(projected_s[rows], pos_ref[...])
        content = query[:, :LANES]
        parts_s[rows, :LANES] = (content + position).astype(BF16)
        return content_sum + fold_rows(content), position_sum + fold_rows(position)

    content_sum, position_sum = lax.fori_loop(0, frames // TALL, score_step, (zero, zero), unroll=4)
    query_ref, n_ref, q_position_ref = query_ref(), n_ref(), q_position_ref()
    qkv_ref, hat_ref = qkv_ref(), hat_ref()
    grad_key = dot_tn(query_ref[...], raw_s[...])
    grad_value = dot_tn(grad_s[...], prob_ref[...])
    for block in range(blocks):
        at = slice(block * BLOCK, (block + 1) * BLOCK)
        parts_s[at, LANES : 2 * LANES] = jnp.transpose(grad_key[:, at]).astype(BF16)
        parts_s[at, 2 * LANES :] = jnp.transpose(grad_value[:, at]).astype(BF16)
    grads_s[:HEAD] = dot_tn(parts_s[:, :LANES], n_ref[...])[:HEAD]
    grads_s[HEAD : 2 * HEAD] = dot_nn(grad_key.astype(BF16), n_ref[...])[:HEAD]
    grads_s[2 * HEAD : 3 * HEAD] = dot_nn(grad_value.astype(BF16), n_ref[...])[:HEAD]
    grads_s[3 * HEAD :] = dot_tn(q_position_ref[...], projected_s[...])[:HEAD]
    stream = lax.axis_index("stream")
    early_ref = early_ref()
    for apart, pack_out in enumerate((pack_0, pack_1, pack_2, pack_3)):
        quarter = lax.bitwise_xor(stream, jnp.int32(apart))
        lanes = pl.ds(pl.multiple_of(quarter * LANES, LANES), LANES)
        pack_out.buffer[: 4 * HEAD] = grads_s[:, lanes].astype(BF16)
        pack_out.buffer[4 * HEAD :] = early_ref[quarter]
        pack_out.go()
    gain = line_of(gain_ref)
    wide_zero = jnp.zeros((8, D), F32)

    def norm_step(block, sums):
        gain_sum, bias_sum = sums
        grad = dot_nt(parts_s[rows_of(block, TALL)], qkv_ref[...])
        for part in range(TALL // 32):
            at = pl.ds(pl.multiple_of(block * TALL + part * 32, 32), 32)
            own = grad[part * 32 : part * 32 + 32]
            total_out.buffer[at] = (own * gain).astype(BF16)
            gain_sum = gain_sum + fold_rows(own * hat_ref[at].astype(F32))
            bias_sum = bias_sum + fold_rows(own)
        return gain_sum, bias_sum

    gain_sum, bias_sum = lax.fori_loop(0, frames // TALL, norm_step, (wide_zero, wide_zero), unroll=4)
    lane = lax.broadcasted_iota(jnp.int32, (1, LANES), 1)

    def own_lanes(sums):
        line = one_row(sums)
        line = line + turn(line)
        tiles = [
            jnp.where(lax.div(tile * LANES + lane, HEAD) == place, line, 0.0) for tile in range(D // LANES)
        ]
        return jnp.concatenate(tiles, axis=1)

    lines_out[...] = jnp.concatenate(
        [
            one_row(gain_sum),
            one_row(bias_sum),
            own_lanes(content_sum),
            own_lanes(position_sum),
            jnp.zeros((4, D), F32),
        ],
        axis=0,
    )


def mlp_second_kernel(
    mixed_ref,
    gate_pre_ref,
    grad_ref,
    rate_ref,
    hat_ref,
    up_ref,
    norm_hat_ref,
    gain_ref,
    other_ref,
    n_ref,
    vectors_ref,
    first_lines_ref,
    head_lines_ref,
    same_out,
    apart_out,
    pack_out,
    pre_s,
    columns_s,
    grad_up_s,
    lines_s,
    up_columns_s,
):
    pack_ref = pack_out.buffer
    place = lax.axis_index("tm")
    frames = pre_s.shape[0]
    half = frames // 2
    blocks = frames // BLOCK
    quarters = pack_ref.shape[0]
    channels = vectors_ref.shape[0]
    share = channels // quarters
    totals = jnp.zeros((2 * blocks, LANES), F32)
    mixed_ref = mixed_ref()
    for source in range(mixed_ref.shape[0]):
        both = mixed_ref[source].astype(F32)
        totals = totals + (both[:, :LANES] + both[:, LANES:])
    totals = totals * (1.0 / HALF)
    columns = jnp.transpose(jnp.concatenate([totals, jnp.zeros((LANES - 2 * blocks, LANES), F32)], axis=0))
    lane = lax.broadcasted_iota(jnp.int32, (BLOCK, LANES), 1)
    for block in range(blocks):
        columns_s[block * BLOCK : (block + 1) * BLOCK] = jnp.where(
            lane == 0, columns[:, 2 * block : 2 * block + 1], columns[:, 2 * block + 1 : 2 * block + 2]
        )
    gate_pre_ref, grad_ref, rate_ref, hat_ref = gate_pre_ref(), grad_ref(), rate_ref(), hat_ref()
    begin(n_ref, up_ref, norm_hat_ref, other_ref)
    low = low_lanes(64)
    gain = line_of(gain_ref)

    def chunk(start, base=0):
        return pl.ds(pl.multiple_of(start, 64) + base, 64)

    def pre_part(rows, table, up_sum):
        plain, along = table
        hat, rate = hat_ref[rows].astype(F32), rate_ref[rows].astype(F32)
        pre = (grad_ref[rows].astype(F32) - rate * (plain + hat * along)).astype(BF16).astype(F32)
        return pre, up_sum + fold_rows(pre)

    def pre_step(block, sums):
        main_up, rest_up = sums
        for part in range(TALL // 64):
            start = block * TALL + part * 64
            tables = []
            for base in (0, half):
                rows = chunk(start, base)
                values = columns_s[rows]
                table = [values[:, item : item + 1] for item in range(2)]
                tables.append(table)
                pre, main_up = pre_part(rows, table, main_up)
                pre_s[rows, :LANES] = gate_pre_ref[rows]
                pre_s[rows, 2 * LANES :] = pre.astype(BF16)
            rows = chunk(start, frames)
            table = [jnp.where(low, one, other) for one, other in zip(*tables)]
            pre, rest_up = pre_part(rows, table, rest_up)
            gate_pre = gate_pre_ref[rows].astype(F32)
            pre_s[chunk(start), LANES : 2 * LANES] = jnp.where(low, gate_pre, turn(pre)).astype(BF16)
            pre_s[chunk(start, half), LANES : 2 * LANES] = jnp.where(low, turn(gate_pre), pre).astype(BF16)
        return main_up, rest_up

    zero = jnp.zeros((8, LANES), F32)
    main_up, rest_up = lax.fori_loop(0, half // TALL, pre_step, (zero, zero), unroll=2)
    n_ref, up_ref, norm_hat_ref, other_ref = n_ref(), up_ref(), norm_hat_ref(), other_ref()
    grad_up_s[...] = dot_tn(pre_s[:, LANES:], n_ref[...])
    wide_zero = jnp.zeros((8, D), F32)

    def norm_step(block, sums):
        gain_sum, bias_sum = sums
        rows = rows_of(block, BLOCK)
        grad = dot_nt(pre_s[rows], up_ref[...])
        total = (grad * gain + other_ref[rows].astype(F32)).astype(BF16)
        apart = lax.bitwise_xor(block, place)

        @pl.when(lax.rem(apart, 2) == 0)
        def _():
            same_out.buffer[lax.div(apart, 2)] = total

        @pl.when(lax.rem(apart, 2) == 1)
        def _():
            apart_out.buffer[lax.div(apart, 2)] = total

        return gain_sum + fold_rows(grad * norm_hat_ref[rows].astype(F32)), bias_sum + fold_rows(grad)

    gain_sum, bias_sum = lax.fori_loop(0, blocks, norm_step, (wide_zero, wide_zero), unroll=4)
    apart_out.go()
    same_out.go()
    rest_line = one_row(rest_up)
    up_columns_s[:LANES] = jnp.transpose(jnp.broadcast_to(one_row(main_up), (LANES, LANES)))
    up_columns_s[LANES:] = jnp.transpose(jnp.broadcast_to(rest_line + turn(rest_line), (LANES, LANES)))[:LOW]
    first_device = (place == 0).astype(F32)
    lines_s[...] = jnp.concatenate(
        [
            head_lines_ref[0:2],
            one_row(gain_sum),
            one_row(bias_sum),
            head_lines_ref[2:4],
            first_lines_ref[0:2] * first_device,
            jnp.zeros((8, D), F32),
        ],
        axis=0,
    )
    gate_at = KERNEL + 3
    lane = lax.broadcasted_iota(jnp.int32, (share, LANES), 1)
    for quarter in range(quarters):
        lanes = slice(quarter * LANES, (quarter + 1) * LANES)
        pack_ref[quarter, :LANES] = grad_up_s[LANES:, lanes].astype(BF16)
        pack_ref[quarter, LANES:channels] = grad_up_s[LOW:LANES, lanes].astype(BF16)
        table = vectors_ref[quarter * share : (quarter + 1) * share]
        for other in range(2):
            at = slice((2 * (quarter % 2) + other) * share, (2 * (quarter % 2) + other + 1) * share)
            column = vectors_ref[at, gate_at : gate_at + 1] if quarter < quarters // 2 else up_columns_s[at, 0:1]
            table = jnp.where(lane == gate_at + other, column, table)
        pack_ref[quarter, channels : channels + share] = table.astype(BF16)
        pack_ref[quarter, channels + share : channels + share + 16] = lines_s[:, lanes].astype(BF16)


def merge_kernel(joined_ref, branch_ref, cot_ref, up_ref, pack_out):
    pack_ref = pack_out.buffer
    cot_ref = cot_ref()
    quarters, first, _ = up_ref.shape
    sources, _, rows = joined_ref.shape
    merge_rows = 2 * D // sources
    head_rows = D // sources
    grad_merge = jnp.zeros((merge_rows, D), F32)
    grad_head = jnp.zeros((head_rows, D), F32)
    for source in range(sources):
        at = slice(source * rows, (source + 1) * rows)
        joined = joined_ref[source]
        grad_merge = grad_merge + dot_nn(joined[:merge_rows], cot_ref[at])
        grad_head = grad_head + dot_nn(joined[merge_rows : merge_rows + head_rows], branch_ref[at])
    pack_ref[:, :first] = up_ref[...]
    for quarter in range(quarters):
        base = first
        for grad in (grad_merge, grad_head):
            share = grad.shape[0] // quarters
            for tile in range(4):
                pack_ref[quarter, base : base + share] = grad[
                    quarter * share : (quarter + 1) * share, tile * LANES : (tile + 1) * LANES
                ].astype(BF16)
                base += share


def output_kernel(
    x_ref, mixed_ref, head_ref, down_ref, down_bias_ref, merge_ref, merge_bias_ref, out_ref, joined_out
):
    sources = mixed_ref.shape[0]
    rows = x_ref.shape[0]
    channels = HALF // sources
    share = channels // 4
    attn_parts = []
    branch_attn = jnp.zeros((rows, D), F32)
    branch_mlp = jnp.zeros((rows, D), F32)
    for source in range(sources):
        attn = turn(mixed_ref[source, :rows, LANES:].astype(F32))[:, :HEAD].astype(BF16)
        attn_parts.append(attn)
        branch_attn = branch_attn + dot_nn(attn, head_ref[source * HEAD : (source + 1) * HEAD])
        down = jnp.concatenate(
            [down_ref[(part * sources + source) * share : (part * sources + source + 1) * share] for part in range(4)],
            axis=0,
        )
        branch_mlp = branch_mlp + dot_nn(mixed_ref[source, :rows, :channels], down)
    joined = jnp.concatenate(
        [branch_attn.astype(BF16), (branch_mlp + line_of(down_bias_ref)).astype(BF16)], axis=1
    )
    result = x_ref[...].astype(F32) + dot_nn(joined, merge_ref[...]) + line_of(merge_bias_ref)
    out_ref[...] = result.astype(BF16)
    turned = jnp.transpose(joined.astype(F32))
    heads = jnp.transpose(jnp.concatenate(attn_parts, axis=1).astype(F32))
    merge_share = turned.shape[0] // (4 * sources)
    head_share = heads.shape[0] // (4 * sources)
    used = 4 * (merge_share + head_share)
    for target in range(sources):
        for part in range(4):
            at = (part * sources + target) * merge_share
            joined_out[target, part * merge_share : (part + 1) * merge_share] = turned[
                at : at + merge_share
            ].astype(BF16)
            at = (part * sources + target) * head_share
            to = 4 * merge_share + part * head_share
            joined_out[target, to : to + head_share] = heads[at : at + head_share].astype(BF16)
        joined_out[target, used:] = jnp.zeros((joined_out.shape[1] - used, rows), BF16)


def pair_kernel(same_ref, other_ref, *out_refs):
    for slot, out_ref in enumerate(out_refs):
        out_ref[...] = (same_ref[slot].astype(F32) + other_ref[slot].astype(F32)).astype(BF16)


def frames_kernel(x_ref, cot_ref, *refs):
    total_refs, out_ref = refs[:-1], refs[-1]
    for part in range(x_ref.shape[0] // 32):
        rows = slice(part * 32, part * 32 + 32)
        inputs = x_ref[rows].astype(F32)
        mean = jnp.mean(inputs, axis=-1, keepdims=True)
        centred = inputs - mean
        rate = lax.rsqrt(jnp.mean(centred * centred, axis=-1, keepdims=True) + EPS)
        hat = centred * rate
        grad = total_refs[0][rows].astype(F32)
        for total_ref in total_refs[1:]:
            grad = grad + total_ref[rows].astype(F32)
        plain = jnp.mean(grad, axis=-1, keepdims=True)
        along = jnp.mean(grad * hat, axis=-1, keepdims=True)
        out_ref[rows] = cot_ref[rows].astype(F32) + rate * (grad - plain - hat * along)


def add_kernel(*refs):
    out_ref = refs[-1]
    first = 0
    for at in range(0, len(refs) - 1, 4):
        total = refs[at][...].astype(F32)
        for ref in refs[at + 1 : at + 4]:
            total = total + ref[...].astype(F32)
        out_ref[first : first + total.shape[0]] = total.astype(BF16)
        first += total.shape[0]


def gather_parts(near_ref, far_ref, all_s):
    place = lax.axis_index("tm")
    for apart in range(all_s.shape[0]):
        part_ref = far_ref if apart % 2 else near_ref
        all_s[lax.bitwise_xor(jnp.int32(apart), place)] = part_ref[apart // 2]


def lines_from(all_s, base, size):
    return jnp.concatenate([all_s[source, base : base + size] for source in range(all_s.shape[0])], axis=0).astype(F32)


def add_streams_kernel(parts_ref, out_ref):
    total = parts_ref[0].astype(F32)
    for source in range(1, parts_ref.shape[0]):
        total = total + parts_ref[source].astype(F32)
    out_ref[...] = total.astype(BF16)


def early_kernel(near_ref, far_ref, qkv_out, pos_out, down_out, up_out, all_s):
    gather_parts(near_ref, far_ref, all_s)
    sources = all_s.shape[0]
    share = HALF // (4 * sources)
    for kind in range(4):
        lines = jnp.transpose(lines_from(all_s, kind * HEAD, HEAD))
        if kind < 3:
            qkv_out[:, kind * D : (kind + 1) * D] = lines
        else:
            pos_out[...] = lines
    base = 4 * HEAD
    for source in range(sources):
        for tile in range(4):
            down_out[source * share : (source + 1) * share, tile * LANES : (tile + 1) * LANES] = all_s[
                source, base + tile * share : base + (tile + 1) * share
            ].astype(F32)
    wide = sources * share
    for group in range(4):
        up_out.buffer[:, group * wide : (group + 1) * wide] = jnp.transpose(
            lines_from(all_s, base + 4 * share + group * share, share)
        )


def late_kernel(*refs):
    _, near_ref, far_ref = refs[:3]
    (
        attn_gain_out,
        attn_bias_out,
        mlp_gain_out,
        mlp_bias_out,
        content_out,
        position_out,
        outw_out,
        up_out,
        up_bias_out,
        gain_out,
        bias_out,
        taps_out,
        conv_bias_out,
        down_bias_out,
        merge_out,
        merge_bias_out,
        all_s,
    ) = refs[3:]
    gather_parts(near_ref, far_ref, all_s)
    sources = all_s.shape[0]
    channels = HALF // sources
    share = channels // 4
    base = 0
    for group in range(4):
        at = group * sources * share
        up_out.buffer[:, at : at + sources * share] = jnp.transpose(lines_from(all_s, base + group * share, share))
    up_out.go()
    table = jnp.transpose(lines_from(all_s, base + channels, share))
    taps_out[...] = table[:KERNEL]
    conv_bias_out[...] = table[KERNEL]
    gain_out[...] = table[KERNEL + 1]
    bias_out[...] = table[KERNEL + 2]
    wide = sources * share
    up_bias_out[:wide] = table[KERNEL + 3]
    up_bias_out[wide:] = table[KERNEL + 4]
    base = base + channels + share
    lines = all_s[0, base : base + 16].astype(F32)
    for source in range(1, sources):
        lines = lines + all_s[source, base : base + 16].astype(F32)
    outs = (attn_gain_out, attn_bias_out, mlp_gain_out, mlp_bias_out, content_out, position_out, down_bias_out, merge_bias_out)
    for line, out in enumerate(outs):
        out[...] = lines[line]
    base = base + 16
    merge_share = 2 * D // (4 * sources)
    head_share = D // (4 * sources)
    for source in range(sources):
        for tile in range(4):
            lanes = slice(tile * LANES, (tile + 1) * LANES)
            at = base + tile * merge_share
            merge_out[source * merge_share : (source + 1) * merge_share, lanes] = all_s[
                source, at : at + merge_share
            ].astype(F32)
            at = base + 4 * merge_share + tile * head_share
            outw_out[source * head_share : (source + 1) * head_share, lanes] = all_s[
                source, at : at + head_share
            ].astype(F32)


def moved(block, axis, bits):
    count = lax.axis_size(axis)
    return lax.ppermute(block, axis, [(index, index ^ bits) for index in range(count)])


def over_streams(packs):
    return [packs[0]] + [moved(packs[bits], "stream", bits) for bits in range(1, lax.axis_size("stream"))]


def near_blocks(block):
    return [block] + [moved(block, "tm", bits) for bits in range(2, lax.axis_size("tm"), 2)]


def far_blocks(near):
    far = [moved(part, "tm", 1) for part in near]
    return [part for pair in zip(near, far) for part in pair]


def far_stack(near):
    stack = jnp.stack(near)
    return stack, moved(stack, "tm", 1)


def head_device(
    frames,
    lengths,
    cotangent,
    ln_attn_gain,
    ln_attn_bias,
    ln_mlp_gain,
    ln_mlp_bias,
    qkv_weight,
    content_bias,
    position_bias,
    pos_weight,
    out_weight,
    up_weight,
    up_bias,
    gate_norm_gain,
    gate_norm_bias,
    conv_kernel,
    conv_bias,
    down_weight,
    down_bias,
    merge_weight,
    merge_bias,
):
    count = lax.axis_size("tm")
    quarters = lax.axis_size("stream")
    own = frames.shape[1]
    total = own * count
    folded = total + total // 2
    padded = folded + 4 * MARGIN
    share = HALF // (quarters * count)
    channels = HALF // count
    quarter = D // quarters
    own_frames = frames[0]
    own_cotangent = cotangent[0]

    whole, late = Part(), Part(late=True)
    near = near_blocks(jnp.concatenate([own_frames, own_cotangent], axis=1))
    up_own, table, qkv_own, pos_own, bias_own = kernel_call(
        select_kernel,
        [
            ((D, 3 * LANES), BF16),
            ((2, 8 + KERNEL + 1, LANES), F32),
            ((D, 3 * LANES), BF16),
            ((D, LANES), BF16),
            ((8, LANES), F32),
        ],
        10 * "v",
    )(
        up_weight,
        up_bias,
        gate_norm_gain,
        gate_norm_bias,
        conv_bias,
        conv_kernel,
        qkv_weight,
        pos_weight,
        content_bias,
        position_bias,
    )
    near, up_own = lax.optimization_barrier((near, up_own))
    blocks = far_blocks(near)
    frequency = jnp.exp(jnp.arange(D // 2, dtype=F32) * (-2.0 * math.log(10000.0) / D))
    coarse = jnp.arange(0, total, BLOCK, dtype=F32)[:, None] * frequency[None]
    fine = jnp.arange(BLOCK, dtype=F32)[:, None] * frequency[None]
    coarse_table = jnp.concatenate([jnp.sin(coarse), jnp.cos(coarse)], axis=1)
    fine_table = jnp.concatenate([jnp.sin(fine), jnp.cos(fine)], axis=1)

    n_attn, n_mlp, hat, q_position, query, key, value, prob, attn, stats = kernel_call(
        attend_kernel,
        [
            ((total, D), BF16, 1),
            ((total, D), BF16, 1),
            ((total, D), BF16, 1),
            ((total, LANES), BF16, 1),
            ((total, LANES + D), BF16, 1),
            ((total, LANES + D), BF16, 1),
            ((total, LANES), BF16, 1),
            ((total, total), BF16, 1),
            ((total, LANES), F32, 1),
            ((total, LANES), F32, 1),
        ],
        [
            "s",
            blocks_part(0),
            *"vvvvvvvvv",
            Part((D, HALF), lambda refs, buffer: [(refs[0].at[:, pl.ds(HALF, HALF)], buffer)], late=True),
            "v",
        ],
        bounds=True,
    )(
        lengths,
        *blocks,
        ln_attn_gain,
        ln_attn_bias,
        ln_mlp_gain,
        ln_mlp_bias,
        qkv_own,
        pos_own,
        bias_own,
        coarse_table,
        fine_table,
        up_weight,
        up_bias,
    )

    def own_down(refs, buffer):
        place = lax.axis_index("tm")
        stride = HALF // quarters
        return [
            (
                refs[0].at[pl.ds(pl.multiple_of(part * stride + share * place, 16), share)],
                buffer.at[pl.ds(part * share, share)],
            )
            for part in range(quarters)
        ]

    mixed, gate_pre, grad_y, slope, gate_hat, early_pack, vectors, first_lines = kernel_call(
        mlp_first_kernel,
        [
            ((count, own + 16, 2 * LANES), BF16, 1),
            ((folded, LANES), BF16, 1),
            ((folded, LANES), BF16, 1),
            ((folded, LANES), BF16, 1),
            ((folded, LANES), BF16, 1),
            ((quarters, 8 * share, LANES), BF16, 1),
            ((channels, LANES), F32),
            ((8, D), F32),
        ],
        [
            "s",
            whole,
            "v",
            "v",
            whole,
            blocks_part(1, late=True),
            rows_part(D, D, late=True),
            Part((2 * LANES, D), own_down, late=True),
            Part(late=True),
        ],
        [
            ((folded, LANES), F32),
            ((folded, LANES), F32),
            ((total, 2 * LANES), BF16),
            ((folded, LANES), F32),
            ((folded, LANES), F32),
            ((8, padded + WINDOW, LANES), F32),
            ((8, padded + WINDOW, LANES), F32),
            ((folded, LANES), F32),
            ((folded, LANES), F32),
            ((total, D), BF16),
            ((total, 2 * LANES), BF16),
            ((2, 32, 8, LANES), F32),
            ((2, 32, 8, LANES), F32),
            ((2, 32, 8, LANES), F32),
            ((total, LANES), F32),
        ],
        bounds=True,
    )(lengths, n_mlp, up_own, table, stats, *blocks, merge_weight, down_weight, attn)
    mixed_own = lax.all_to_all(mixed, "tm", 0, 0, tiled=True)

    def own_head(refs, buffer):
        at = pl.ds(pl.multiple_of(lax.axis_index("tm") * HEAD, HEAD), HEAD)
        return [(refs[0].at[at], buffer.at[pl.ds(0, HEAD)])]

    branch, from_attn, *head_packs, head_lines = kernel_call(
        attend_back_kernel,
        [
            ((total, D), BF16, 1),
            ((total, D), BF16, 1),
            *([((4 * HEAD + 8 * share, LANES), BF16, 1)] * quarters),
            ((8, D), F32),
        ],
        [
            blocks_part(1),
            rows_part(0, D),
            Part((LANES, D), own_head),
            whole,
            late,
            late,
            late,
            "v",
            "v",
            late,
            Part((total, LANES), lambda refs, buffer: [(refs[0].at[:, pl.ds(0, LANES)], buffer)], late=True),
            late,
            late,
            late,
            late,
            "v",
            late,
        ],
        [
            ((total, LANES), BF16),
            ((total, total), BF16),
            ((total, D), BF16),
            ((total, 3 * LANES), BF16),
            ((4 * HEAD, D), F32),
        ],
    )(
        *blocks,
        merge_weight,
        out_weight,
        attn,
        value,
        prob,
        key,
        coarse_table,
        fine_table,
        pos_own,
        query,
        n_attn,
        q_position,
        qkv_own,
        hat,
        ln_attn_gain,
        early_pack,
    )
    head_parts = over_streams(head_packs)
    mixed_own, _ = lax.optimization_barrier((mixed_own, head_lines))
    out_rows, joined = kernel_call(
        output_kernel,
        [((own, D), BF16), ((count, 256, own), BF16)],
        "vvvvvvv",
        megas=24,
    )(own_frames, mixed_own, out_weight, down_weight, down_bias, merge_weight, merge_bias)
    joined_all = lax.all_to_all(joined, "tm", 0, 0, tiled=True)
    gate_pre, _ = lax.optimization_barrier((gate_pre, joined))
    up_rows = 5 * share + 16
    late_rows = up_rows + 3 * D // count
    same, apart, up_pack = kernel_call(
        mlp_second_kernel,
        [((count // 2, own, D), BF16, 1)] * 2 + [((quarters, up_rows, LANES), BF16, 1)],
        [
            Part(
                (count, 2 * total // BLOCK, 2 * LANES),
                lambda refs, buffer: [(refs[0].at[:, pl.ds(own, 2 * total // BLOCK)], buffer)],
            ),
            *([whole] * 4),
            late,
            late,
            "v",
            late,
            late,
            *"vvv",
        ],
        [
            ((total, 3 * LANES), BF16),
            ((total, LANES), F32),
            ((2 * LANES, D), F32),
            ((16, D), F32),
            ((channels, LANES), F32),
        ],
    )(
        mixed_own,
        gate_pre,
        grad_y,
        slope,
        gate_hat,
        up_own,
        hat,
        ln_mlp_gain,
        from_attn,
        n_mlp,
        vectors,
        first_lines,
        head_lines,
    )
    (late_pack,) = kernel_call(
        merge_kernel, [((quarters, late_rows, LANES), BF16, 1)], ["f", "f", blocks_part(1), "f"]
    )(joined_all, branch, *blocks, up_pack)
    late_pack, head_parts = lax.optimization_barrier((late_pack, head_parts))
    late_moved = lax.all_to_all(late_pack, "stream", 0, 0, tiled=True)
    sibling = moved(apart, "tm", 1)
    (early_part,) = kernel_call(add_kernel, [((4 * HEAD + 8 * share, LANES), BF16)], quarters * "v", megas=24)(
        *head_parts
    )
    early_near = near_blocks(early_part)
    pairs = kernel_call(pair_kernel, [((own, D), BF16)] * (count // 2), "vv", megas=24)(same, sibling)
    sums = [pairs[0]] + [moved(pairs[slot], "tm", 2 * slot) for slot in range(1, count // 2)]
    late_moved, early_near, sums = lax.optimization_barrier((late_moved, early_near, sums))
    (late_part,) = kernel_call(add_streams_kernel, [((late_rows, LANES), BF16)], "v", megas=24)(late_moved)
    late_near = near_blocks(late_part)
    early_all = far_stack(early_near)
    (grad_frames,) = kernel_call(frames_kernel, [((own, D), F32)], (2 + count // 2) * "v", megas=24)(
        own_frames, own_cotangent, *sums
    )
    grad_qkv, grad_pos, grad_down, half_up = kernel_call(
        early_kernel,
        [
            ((quarter, 3 * D), F32),
            ((quarter, D), F32),
            ((HALF // quarters, D), F32),
            ((quarter, 2 * HALF), F32, 1, (quarter, HALF), lambda ref: ref.at[:, pl.ds(0, HALF)]),
        ],
        "vv",
        [((count, 4 * HEAD + 8 * share, LANES), BF16)],
        megas=24,
    )(*early_all)
    late_near, grad_frames, grad_pos = lax.optimization_barrier((late_near, grad_frames, grad_pos))
    late_parts = far_stack(late_near)
    late = kernel_call(
        late_kernel,
        [((quarter,), F32)] * 6
        + [
            ((quarter, D), F32),
            ((quarter, 2 * HALF), F32, 1, (quarter, HALF), lambda ref: ref.at[:, pl.ds(HALF, HALF)]),
            ((2 * HALF // quarters,), F32),
            ((HALF // quarters,), F32),
            ((HALF // quarters,), F32),
            ((KERNEL, HALF // quarters), F32),
            ((HALF // quarters,), F32),
            ((quarter,), F32),
            ((2 * D // quarters, D), F32),
            ((quarter,), F32),
        ],
        "kvv",
        [((count,) + late_part.shape, BF16)],
        megas=24,
        aliases={0: 7},
    )(half_up, *late_parts)
    return (
        out_rows[None],
        grad_frames[None],
        *late[:4],
        grad_qkv,
        *late[4:6],
        grad_pos,
        *late[6:13],
        grad_down,
        *late[13:],
    )


def per_device(*operands):
    fits = (
        lax.axis_size("tm") == HEADS
        and lax.axis_size("stream") * LANES == D
        and operands[0].shape[1] == BLOCK
    )
    return head_device(*operands) if fits else frame_device(*operands)


def solution(mesh):
    return jax.shard_map(
        per_device,
        mesh=mesh,
        in_specs=(
            P("stream", "tm", None),
            P("stream", None),
            P("stream", "tm", None),
            P(),
            P(),
            P(),
            P(),
            P(),
            P(),
            P(),
            P(),
            P(),
            P(),
            P(),
            P(),
            P(),
            P(),
            P(),
            P(),
            P(),
            P(),
            P(),
        ),
        out_specs=(
            P("stream", "tm", None),
            P("stream", "tm", None),
            P("stream"),
            P("stream"),
            P("stream"),
            P("stream"),
            P("stream", None),
            P("stream"),
            P("stream"),
            P("stream", None),
            P("stream", None),
            P("stream", None),
            P("stream"),
            P("stream"),
            P("stream"),
            P(None, "stream"),
            P("stream"),
            P("stream", None),
            P("stream"),
            P("stream", None),
            P("stream"),
        ),
        check_vma=False,
    )
```

```python
import math

import jax
import jax.numpy as jnp
from jax import lax
from jax.experimental import pallas as pl
from jax.experimental.pallas import tpu as pltpu
from jax.sharding import PartitionSpec as P

D = 512
HEADS = 8
HEAD = 64
KERNEL = 31
ITEMS = 5
HALF = 1536


EPS = 1e-05
MASKED = -1e30


def extended(block, sides, width):
    for axis, dim in sides:
        count = lax.axis_size(axis)
        forward = [(i, i + 1) for i in range(count - 1)]
        backward = [(target, source) for source, target in forward]
        low = lax.ppermute(
            lax.slice_in_dim(block, block.shape[dim] - width, None, axis=dim), axis, forward
        )
        high = lax.ppermute(lax.slice_in_dim(block, 0, width, axis=dim), axis, backward)
        block = jnp.concatenate([low, block, high], axis=dim)
    return block


def norm_rows(inputs, scale_row, shift_row):
    row_mean = jnp.mean(inputs, axis=-1, keepdims=True)
    centred = inputs - row_mean
    spread = jnp.mean(centred * centred, axis=-1, keepdims=True)
    return centred * lax.rsqrt(spread + EPS) * scale_row + shift_row


def gelu_exact(inputs):
    return jax.nn.gelu(inputs, approximate=False)


def frame_info(lengths, offset, extent):
    item_ends = jnp.cumsum(lengths)
    first_table = jnp.concatenate([item_ends - lengths, item_ends[-1:]])
    frame_index = offset + jnp.arange(extent, dtype=jnp.int32)
    item_of = jnp.sum((frame_index[:, None] >= item_ends[None, :]).astype(jnp.int32), axis=1)
    labels = jnp.arange(ITEMS + 1, dtype=jnp.int32)
    first_frame = jnp.sum(
        jnp.where(item_of[:, None] == labels[None, :], first_table[None, :], 0), axis=1
    )
    return (frame_index, item_of, frame_index - first_frame)


def angles(place_in):
    frequency = jnp.exp(jnp.arange(D // 2, dtype=jnp.float32) * (-2.0 * math.log(10000.0) / D))
    phase_angle = place_in.astype(jnp.float32)[:, None] * frequency[None, :]
    return (jnp.sin(phase_angle), jnp.cos(phase_angle))


def rel_query(projected, sine_rows, cosine_rows):
    half_size = projected.shape[-1] // 2
    first_half = projected[..., :half_size]
    second_half = projected[..., half_size:]
    sine_wide = sine_rows[:, None, :]
    cosine_wide = cosine_rows[:, None, :]
    return jnp.concatenate(
        [
            first_half * sine_wide + second_half * cosine_wide,
            second_half * sine_wide - first_half * cosine_wide,
        ],
        axis=-1,
    )


def step_size(extent):
    return math.gcd(extent, 512)


def score_block(q_content, q_rel, query_item, query_frame, key_block, key_start, lengths):
    extent = key_block.shape[0]
    key_frame, key_item, key_place = frame_info(lengths, key_start, extent)
    sine_rows, cosine_rows = angles(key_place)
    k_rel = jnp.concatenate([cosine_rows, sine_rows], axis=1).astype(jnp.bfloat16)
    raw_scores = jnp.einsum(
        "qhe,khe->hqk",
        q_content,
        key_block.reshape(extent, HEADS, HEAD),
        preferred_element_type=jnp.float32,
    )
    raw_scores = raw_scores + jnp.einsum(
        "qhc,kc->hqk", q_rel, k_rel, preferred_element_type=jnp.float32
    )
    allowed = (query_item[:, None] == key_item[None, :]) & (
        (query_item[:, None] < ITEMS) | (query_frame[:, None] == key_frame[None, :])
    )
    return (raw_scores, allowed, k_rel)


def block_grads(
    q_content,
    q_rel,
    query_item,
    query_frame,
    grad_out,
    log_total,
    delta_rows,
    key_block,
    value_block,
    key_start,
    lengths,
):
    extent = key_block.shape[0]
    raw_scores, allowed, k_rel = score_block(
        q_content, q_rel, query_item, query_frame, key_block, key_start, lengths
    )
    prob_rows = jnp.where(allowed[None], jnp.exp(raw_scores * 0.125 - log_total[:, :, None]), 0.0)
    grad_prob = jnp.einsum(
        "qhe,khe->hqk",
        grad_out,
        value_block.reshape(extent, HEADS, HEAD),
        preferred_element_type=jnp.float32,
    )
    grad_raw = (prob_rows * (grad_prob - delta_rows[:, :, None]) * 0.125).astype(jnp.bfloat16)
    return (prob_rows.astype(jnp.bfloat16), grad_raw, k_rel)


def frame_device(
    frames,
    lengths,
    cotangent,
    ln_attn_gain,
    ln_attn_bias,
    ln_mlp_gain,
    ln_mlp_bias,
    qkv_weight,
    content_bias,
    position_bias,
    pos_weight,
    out_weight,
    up_weight,
    up_bias,
    gate_norm_gain,
    gate_norm_bias,
    conv_kernel,
    conv_bias,
    down_weight,
    down_bias,
    merge_weight,
    merge_bias,
):
    row_count = frames.shape[1]
    cycle_size = lax.axis_size("tm")
    offset = lax.axis_index("tm") * row_count
    stream_lengths = lengths[0]
    inputs = frames[0].astype(jnp.float32)
    frame_index, item_of, place_in = frame_info(stream_lengths, offset, row_count)
    sine_rows, cosine_rows = angles(place_in)
    attn_norm, attn_pull = jax.vjp(
        norm_rows, inputs, ln_attn_gain.astype(jnp.float32), ln_attn_bias.astype(jnp.float32)
    )
    mlp_norm, mlp_pull = jax.vjp(
        norm_rows, inputs, ln_mlp_gain.astype(jnp.float32), ln_mlp_bias.astype(jnp.float32)
    )
    attn_norm_low = attn_norm.astype(jnp.bfloat16)
    mlp_norm_low = mlp_norm.astype(jnp.bfloat16)
    qkv_rows = jnp.dot(attn_norm_low, qkv_weight, preferred_element_type=jnp.float32)
    query_rows = qkv_rows[:, :D]
    key_rows = qkv_rows[:, D : 2 * D].astype(jnp.bfloat16)
    value_rows = qkv_rows[:, 2 * D :].astype(jnp.bfloat16)
    q_content = (query_rows + content_bias.astype(jnp.float32)).astype(jnp.bfloat16)
    q_position = (query_rows + position_bias.astype(jnp.float32)).astype(jnp.bfloat16)
    content_heads = q_content.reshape(row_count, HEADS, HEAD)
    position_heads = q_position.reshape(row_count, HEADS, HEAD)
    pos_heads = pos_weight.reshape(D, HEADS, HEAD)
    projected = jnp.einsum(
        "the,che->thc", position_heads, pos_heads, preferred_element_type=jnp.float32
    )
    q_rel = rel_query(projected, sine_rows, cosine_rows).astype(jnp.bfloat16)
    start_state = (
        jnp.full((HEADS, row_count), MASKED, jnp.float32),
        jnp.zeros((HEADS, row_count), jnp.float32),
        jnp.zeros((HEADS, row_count, HEAD), jnp.float32),
    )
    fold_state = start_state
    key_piece = lax.all_gather(key_rows, "tm", axis=0, tiled=True)
    value_piece = lax.all_gather(value_rows, "tm", axis=0, tiled=True)
    extent = key_piece.shape[0]
    step_rows = step_size(extent)

    def forward_one_step(inner_state, step_index):
        row_top, row_total, row_acc = inner_state
        key_block = lax.dynamic_slice_in_dim(key_piece, step_index * step_rows, step_rows, 0)
        value_block = lax.dynamic_slice_in_dim(value_piece, step_index * step_rows, step_rows, 0)
        raw_scores, allowed, k_rel = score_block(
            content_heads,
            q_rel,
            item_of,
            frame_index,
            key_block,
            step_index * step_rows,
            stream_lengths,
        )
        scaled = jnp.where(allowed[None], raw_scores * 0.125, MASKED)
        new_top = jnp.maximum(row_top, jnp.max(scaled, axis=2))
        weight = jnp.where(allowed[None], jnp.exp(scaled - new_top[:, :, None]), 0.0)
        factor = jnp.exp(row_top - new_top)
        row_total = row_total * factor + jnp.sum(weight, axis=2)
        row_acc = row_acc * factor[:, :, None] + jnp.einsum(
            "hqk,khe->hqe",
            weight.astype(jnp.bfloat16),
            value_block.reshape(step_rows, HEADS, HEAD),
            preferred_element_type=jnp.float32,
        )
        return ((new_top, row_total, row_acc), None)

    fold_state, unused = lax.scan(
        forward_one_step, fold_state, jnp.arange(extent // step_rows, dtype=jnp.int32)
    )
    row_top, row_total, row_acc = fold_state
    attn_heads = row_acc / row_total[:, :, None]
    log_total = row_top + jnp.log(row_total)
    attn_low = jnp.transpose(attn_heads, (1, 0, 2)).reshape(row_count, D).astype(jnp.bfloat16)
    branch_attn = jnp.dot(attn_low, out_weight, preferred_element_type=jnp.float32).astype(
        jnp.bfloat16
    )
    hidden_pre = jnp.dot(
        mlp_norm_low, up_weight, preferred_element_type=jnp.float32
    ) + up_bias.astype(jnp.float32)
    hidden, gelu_pull = jax.vjp(gelu_exact, hidden_pre)
    gate_half = hidden[:, :HALF]
    conv_norm, conv_pull = jax.vjp(
        norm_rows,
        hidden[:, HALF:],
        gate_norm_gain.astype(jnp.float32),
        gate_norm_bias.astype(jnp.float32),
    )
    conv_in = conv_norm.astype(jnp.bfloat16)
    half_width = KERNEL // 2
    conv_wide = extended(conv_in, (("tm", 0),), half_width)
    wide_frame, wide_item, wide_place = frame_info(
        stream_lengths, offset - half_width, row_count + 2 * half_width
    )
    kernel_rows = conv_kernel.astype(jnp.float32)
    conv_out = conv_bias.astype(jnp.float32) + jnp.zeros_like(gate_half)
    for tap_index in range(KERNEL):
        same_item = (wide_item[tap_index : tap_index + row_count] == item_of)[:, None]
        conv_out = (
            conv_out
            + jnp.where(
                same_item, conv_wide[tap_index : tap_index + row_count].astype(jnp.float32), 0.0
            )
            * kernel_rows[tap_index]
        )
    gated_low = (gate_half * conv_out).astype(jnp.bfloat16)
    branch_mlp = (
        jnp.dot(gated_low, down_weight, preferred_element_type=jnp.float32)
        + down_bias.astype(jnp.float32)
    ).astype(jnp.bfloat16)
    joined = jnp.concatenate([branch_attn, branch_mlp], axis=1)
    result = (
        inputs
        + jnp.dot(joined, merge_weight, preferred_element_type=jnp.float32)
        + merge_bias.astype(jnp.float32)
    )
    out_rows = result.astype(jnp.bfloat16)[None]
    grad_low = cotangent[0]
    grad_rows = grad_low.astype(jnp.float32)
    grad_merge_bias = jnp.sum(grad_rows, axis=0)
    grad_merge_weight = jnp.einsum(
        "tc,td->cd", joined, grad_low, preferred_element_type=jnp.float32
    )
    grad_joined = jnp.einsum(
        "td,cd->tc", grad_low, merge_weight, preferred_element_type=jnp.float32
    )
    grad_attn_branch = grad_joined[:, :D].astype(jnp.bfloat16)
    grad_mlp_branch = grad_joined[:, D:].astype(jnp.bfloat16)
    grad_down_weight = jnp.einsum(
        "tc,td->cd", gated_low, grad_mlp_branch, preferred_element_type=jnp.float32
    )
    grad_down_bias = jnp.sum(grad_mlp_branch.astype(jnp.float32), axis=0)
    grad_gated = jnp.einsum(
        "td,cd->tc", grad_mlp_branch, down_weight, preferred_element_type=jnp.float32
    )
    grad_gate_half = grad_gated * conv_out
    grad_conv_out = (grad_gated * gate_half).astype(jnp.bfloat16)
    grad_conv_rows = grad_conv_out.astype(jnp.float32)
    grad_conv_bias = jnp.sum(grad_conv_rows, axis=0)
    grad_wide = extended(grad_conv_out, (("tm", 0),), half_width)
    kernel_list = []
    grad_conv_in = jnp.zeros_like(grad_conv_rows)
    for tap_index in range(KERNEL):
        same_item = (wide_item[tap_index : tap_index + row_count] == item_of)[:, None]
        kernel_list.append(
            jnp.sum(
                jnp.where(
                    same_item, conv_wide[tap_index : tap_index + row_count].astype(jnp.float32), 0.0
                )
                * grad_conv_rows,
                axis=0,
            )
        )
        back_start = 2 * half_width - tap_index
        back_item = (wide_item[back_start : back_start + row_count] == item_of)[:, None]
        grad_conv_in = (
            grad_conv_in
            + jnp.where(
                back_item, grad_wide[back_start : back_start + row_count].astype(jnp.float32), 0.0
            )
            * kernel_rows[tap_index]
        )
    grad_conv_kernel = jnp.stack(kernel_list)
    grad_second, grad_gate_norm_gain, grad_gate_norm_bias = conv_pull(grad_conv_in)
    (grad_pre_rows,) = gelu_pull(jnp.concatenate([grad_gate_half, grad_second], axis=1))
    grad_pre = grad_pre_rows.astype(jnp.bfloat16)
    grad_up_bias = jnp.sum(grad_pre.astype(jnp.float32), axis=0)
    grad_up_weight = jnp.einsum(
        "tc,tf->cf", mlp_norm_low, grad_pre, preferred_element_type=jnp.float32
    )
    grad_mlp_norm = jnp.einsum("tf,cf->tc", grad_pre, up_weight, preferred_element_type=jnp.float32)
    grad_out_weight = jnp.einsum(
        "tc,td->cd", attn_low, grad_attn_branch, preferred_element_type=jnp.float32
    )
    grad_attn_low = jnp.einsum(
        "td,cd->tc", grad_attn_branch, out_weight, preferred_element_type=jnp.float32
    ).astype(jnp.bfloat16)
    grad_out_heads = grad_attn_low.reshape(row_count, HEADS, HEAD)
    delta_rows = jnp.sum(
        jnp.transpose(grad_out_heads.astype(jnp.float32), (1, 0, 2)) * attn_heads, axis=2
    )
    total_frames = row_count * cycle_size
    back_start_state = (
        jnp.zeros((row_count, HEADS, HEAD), jnp.float32),
        jnp.zeros((row_count, HEADS, D), jnp.float32),
        jnp.zeros((total_frames, D), jnp.float32),
        jnp.zeros((total_frames, D), jnp.float32),
    )
    back_key_piece = lax.all_gather(key_rows, "tm", axis=0, tiled=True)
    back_value_piece = lax.all_gather(value_rows, "tm", axis=0, tiled=True)
    extent = back_key_piece.shape[0]
    back_step_rows = step_size(extent)

    def back_one_step(inner_state, step_index):
        grad_content, grad_rel = inner_state
        key_block = lax.dynamic_slice_in_dim(
            back_key_piece, step_index * back_step_rows, back_step_rows, 0
        )
        value_block = lax.dynamic_slice_in_dim(
            back_value_piece, step_index * back_step_rows, back_step_rows, 0
        )
        prob_low, grad_raw, k_rel = block_grads(
            content_heads,
            q_rel,
            item_of,
            frame_index,
            grad_out_heads,
            log_total,
            delta_rows,
            key_block,
            value_block,
            step_index * back_step_rows,
            stream_lengths,
        )
        grad_content = grad_content + jnp.einsum(
            "hqk,khe->qhe",
            grad_raw,
            key_block.reshape(back_step_rows, HEADS, HEAD),
            preferred_element_type=jnp.float32,
        )
        grad_rel = grad_rel + jnp.einsum(
            "hqk,kc->qhc", grad_raw, k_rel, preferred_element_type=jnp.float32
        )
        key_part = jnp.einsum(
            "hqk,qhe->khe", grad_raw, content_heads, preferred_element_type=jnp.float32
        ).reshape(back_step_rows, D)
        value_part = jnp.einsum(
            "hqk,qhe->khe", prob_low, grad_out_heads, preferred_element_type=jnp.float32
        ).reshape(back_step_rows, D)
        return ((grad_content, grad_rel), (key_part, value_part))

    inner_state, block_parts = lax.scan(
        back_one_step,
        (back_start_state[0], back_start_state[1]),
        jnp.arange(extent // back_step_rows, dtype=jnp.int32),
    )
    key_all = block_parts[0].reshape(extent, D)
    value_all = block_parts[1].reshape(extent, D)
    grad_content, grad_rel, key_all, value_all = (
        inner_state[0],
        inner_state[1],
        key_all,
        value_all,
    )
    grad_keys, grad_values = (
        lax.psum_scatter(key_all, "tm", scatter_dimension=0, tiled=True),
        lax.psum_scatter(value_all, "tm", scatter_dimension=0, tiled=True),
    )
    half_size = D // 2
    rel_first = grad_rel[..., :half_size]
    rel_second = grad_rel[..., half_size:]
    sine_wide = sine_rows[:, None, :]
    cosine_wide = cosine_rows[:, None, :]
    grad_projected = jnp.concatenate(
        [
            rel_first * sine_wide - rel_second * cosine_wide,
            rel_first * cosine_wide + rel_second * sine_wide,
        ],
        axis=-1,
    ).astype(jnp.bfloat16)
    grad_pos_weight = jnp.einsum(
        "thc,the->che", grad_projected, position_heads, preferred_element_type=jnp.float32
    ).reshape(D, D)
    grad_q_position = jnp.einsum(
        "thc,che->the", grad_projected, pos_heads, preferred_element_type=jnp.float32
    )
    grad_content_bias = jnp.sum(grad_content, axis=0).reshape(D)
    grad_position_bias = jnp.sum(grad_q_position, axis=0).reshape(D)
    grad_query = (grad_content + grad_q_position).reshape(row_count, D).astype(jnp.bfloat16)
    grad_qkv = jnp.concatenate(
        [grad_query, grad_keys.astype(jnp.bfloat16), grad_values.astype(jnp.bfloat16)], axis=1
    )
    grad_qkv_weight = jnp.einsum(
        "tc,tf->cf", attn_norm_low, grad_qkv, preferred_element_type=jnp.float32
    )
    grad_attn_norm = jnp.einsum(
        "tf,cf->tc", grad_qkv, qkv_weight, preferred_element_type=jnp.float32
    )
    grad_from_attn, grad_ln_attn_gain, grad_ln_attn_bias = attn_pull(grad_attn_norm)
    grad_from_mlp, grad_ln_mlp_gain, grad_ln_mlp_bias = mlp_pull(grad_mlp_norm)
    grad_inputs = grad_rows + grad_from_attn + grad_from_mlp
    weight_grads = (
        grad_ln_attn_gain,
        grad_ln_attn_bias,
        grad_ln_mlp_gain,
        grad_ln_mlp_bias,
        grad_qkv_weight,
        grad_content_bias,
        grad_position_bias,
        grad_pos_weight,
        grad_out_weight,
        grad_up_weight,
        grad_up_bias,
        grad_gate_norm_gain,
        grad_gate_norm_bias,
        grad_conv_kernel,
        grad_conv_bias,
        grad_down_weight,
        grad_down_bias,
        grad_merge_weight,
        grad_merge_bias,
    )
    summed = lax.psum(
        (
            weight_grads[0],
            weight_grads[1],
            weight_grads[2],
            weight_grads[3],
            weight_grads[4],
            weight_grads[5],
            weight_grads[6],
            weight_grads[7],
            weight_grads[8],
            weight_grads[9],
            weight_grads[10],
            weight_grads[11],
            weight_grads[12],
            weight_grads[13],
            weight_grads[14],
            weight_grads[15],
            weight_grads[16],
            weight_grads[17],
            weight_grads[18],
        ),
        "tm",
    )
    shares = (
        lax.psum_scatter(
            summed[0].astype(jnp.bfloat16), "stream", scatter_dimension=0, tiled=True
        ).astype(jnp.float32),
        lax.psum_scatter(
            summed[1].astype(jnp.bfloat16), "stream", scatter_dimension=0, tiled=True
        ).astype(jnp.float32),
        lax.psum_scatter(
            summed[2].astype(jnp.bfloat16), "stream", scatter_dimension=0, tiled=True
        ).astype(jnp.float32),
        lax.psum_scatter(
            summed[3].astype(jnp.bfloat16), "stream", scatter_dimension=0, tiled=True
        ).astype(jnp.float32),
        lax.psum_scatter(
            summed[4].astype(jnp.bfloat16), "stream", scatter_dimension=0, tiled=True
        ).astype(jnp.float32),
        lax.psum_scatter(
            summed[5].astype(jnp.bfloat16), "stream", scatter_dimension=0, tiled=True
        ).astype(jnp.float32),
        lax.psum_scatter(
            summed[6].astype(jnp.bfloat16), "stream", scatter_dimension=0, tiled=True
        ).astype(jnp.float32),
        lax.psum_scatter(
            summed[7].astype(jnp.bfloat16), "stream", scatter_dimension=0, tiled=True
        ).astype(jnp.float32),
        lax.psum_scatter(
            summed[8].astype(jnp.bfloat16), "stream", scatter_dimension=0, tiled=True
        ).astype(jnp.float32),
        lax.psum_scatter(
            summed[9].astype(jnp.bfloat16), "stream", scatter_dimension=0, tiled=True
        ).astype(jnp.float32),
        lax.psum_scatter(
            summed[10].astype(jnp.bfloat16), "stream", scatter_dimension=0, tiled=True
        ).astype(jnp.float32),
        lax.psum_scatter(
            summed[11].astype(jnp.bfloat16), "stream", scatter_dimension=0, tiled=True
        ).astype(jnp.float32),
        lax.psum_scatter(
            summed[12].astype(jnp.bfloat16), "stream", scatter_dimension=0, tiled=True
        ).astype(jnp.float32),
        lax.psum_scatter(
            summed[13].astype(jnp.bfloat16), "stream", scatter_dimension=1, tiled=True
        ).astype(jnp.float32),
        lax.psum_scatter(
            summed[14].astype(jnp.bfloat16), "stream", scatter_dimension=0, tiled=True
        ).astype(jnp.float32),
        lax.psum_scatter(
            summed[15].astype(jnp.bfloat16), "stream", scatter_dimension=0, tiled=True
        ).astype(jnp.float32),
        lax.psum_scatter(
            summed[16].astype(jnp.bfloat16), "stream", scatter_dimension=0, tiled=True
        ).astype(jnp.float32),
        lax.psum_scatter(
            summed[17].astype(jnp.bfloat16), "stream", scatter_dimension=0, tiled=True
        ).astype(jnp.float32),
        lax.psum_scatter(
            summed[18].astype(jnp.bfloat16), "stream", scatter_dimension=0, tiled=True
        ).astype(jnp.float32),
    )
    return (out_rows, grad_inputs[None]) + tuple(shares)


LANES = 128
LOW = LANES // 2
BLOCK = 128
TALL = 256
WINDOW = 64
MARGIN = 16
BOUNDS = 16
MEGA = 1024 * 1024
F32 = jnp.float32
BF16 = jnp.bfloat16


def dot_nn(left, right):
    return jnp.dot(left, right, preferred_element_type=F32)


def dot_nt(left, right):
    return lax.dot_general(left, right, (((1,), (1,)), ((), ())), preferred_element_type=F32)


def dot_tn(left, right):
    return lax.dot_general(left, right, (((0,), (0,)), ((), ())), preferred_element_type=F32)


def rows_of(index, size, base=0):
    return pl.ds(pl.multiple_of(index * size, size) + base, size)


def line_of(ref):
    return ref[...].astype(F32).reshape(1, ref.shape[0])


def fold_rows(values):
    return jnp.sum(values.reshape(values.shape[0] // 8, 8, values.shape[1]), axis=0)


def one_row(values):
    return jnp.sum(values, axis=0, keepdims=True)


def turn(values):
    return pltpu.roll(values, LOW, 1)


def low_lanes(rows):
    return lax.broadcasted_iota(jnp.int32, (rows, LANES), 1) < LOW


def centre_rows(inputs):
    mean = jnp.mean(inputs, axis=-1, keepdims=True)
    centred = inputs - mean
    spread = jnp.mean(centred * centred, axis=-1, keepdims=True)
    return centred * lax.rsqrt(spread + EPS)


def gelu_parts(values):
    phi = 0.5 + 0.5 * lax.erf(values * math.sqrt(0.5))
    bell = jnp.exp(values * values * -0.5)
    return values * phi, phi + values * bell * (1.0 / math.sqrt(2.0 * math.pi))


class Part:
    def __init__(self, shape=None, pairs=None, refs=1, late=False):
        self.shape, self.pairs, self.refs, self.late = shape, pairs, refs, late

    def buffer(self, operand):
        return self.shape or operand.shape

    def copies(self, refs, buffer):
        return self.pairs(refs, buffer) if self.pairs else [(refs[0], buffer)]


def blocks_part(half, late=False):
    def pairs(refs, buffer):
        place = lax.axis_index("tm")
        return [
            (
                ref.at[:, pl.ds(half * D, D)],
                buffer.at[rows_of(lax.bitwise_xor(jnp.int32(apart), place), BLOCK)],
            )
            for apart, ref in enumerate(refs)
        ]

    return Part((HEADS * BLOCK, D), pairs, HEADS, late)


def rows_part(first, size, late=False):
    return Part((size, D), lambda refs, buffer: [(refs[0].at[pl.ds(first, size)], buffer)], late=late)


class Fetch:
    def __init__(self, pairs, buffer, sems, first):
        self.buffer, self.begun = buffer, False
        self.pending = [
            pltpu.make_async_copy(source, target, sems.at[first + index])
            for index, (source, target) in enumerate(pairs)
        ]

    def begin(self):
        if not self.begun:
            for copy in self.pending:
                copy.start()
        self.begun = True

    def __call__(self):
        self.begin()
        for copy in self.pending:
            copy.wait()
        self.pending = []
        return self.buffer


def begin(*fetches):
    for fetch in fetches:
        fetch.begin()


class Send:
    def __init__(self, buffer, target, sems):
        self.buffer, self.target, self.sems, self.copies = buffer, target, sems, []

    def go(self, *index):
        source, target = (self.buffer.at[index], self.target.at[index]) if index else (self.buffer, self.target)
        copy = pltpu.make_async_copy(source, target, self.sems[len(self.copies)])
        copy.start()
        self.copies.append(copy)

    def finish(self):
        if not self.copies:
            self.go()


SPACES = {"v": pltpu.VMEM, "s": pltpu.SMEM, "k": pl.ANY}


def kernel_call(body, out_shapes, plan, scratch=(), megas=58, bounds=False, aliases=None):
    def call(*operands):
        in_specs, buffers, at = [], [], 0
        for item in plan:
            if item == "f":
                in_specs.append(pl.BlockSpec(memory_space=pl.ANY))
                buffers.append(pltpu.VMEM(operands[at].shape, operands[at].dtype))
                at += 1
            elif isinstance(item, Part):
                in_specs += [pl.BlockSpec(memory_space=pl.ANY)] * item.refs
                buffers.append(pltpu.VMEM(item.buffer(operands[at]), operands[at].dtype))
                at += item.refs
            else:
                in_specs.append(pl.BlockSpec(memory_space=SPACES[item]))
                at += 1
        sent = [out for out in out_shapes if len(out) > 2]
        buffers += [pltpu.VMEM(out[3] if len(out) > 3 else out[0], out[1]) for out in sent]
        sem_count = 96
        extra = [pltpu.SMEM((BOUNDS,), jnp.int32)] if bounds else []

        def outer(*refs):
            inputs, rest = refs[: len(in_specs)], refs[len(in_specs) :]
            outputs, rest = rest[: len(out_shapes)], rest[len(out_shapes) :]
            held, rest = list(rest[: len(buffers)]), rest[len(buffers) :]
            sems, rest = rest[0], rest[1:]
            given, at, used = [], 0, 0
            for item in plan:
                if item == "f":
                    given.append(Fetch([(inputs[at], held[0])], held.pop(0), sems, used))
                    given[-1].begin()
                    used += 1
                    at += 1
                elif isinstance(item, Part):
                    buffer = held.pop(0)
                    pairs = item.copies(inputs[at : at + item.refs], buffer)
                    given.append(Fetch(pairs, buffer, sems, used))
                    if not item.late:
                        given[-1].begin()
                    used += len(pairs)
                    at += item.refs
                else:
                    given.append(inputs[at])
                    at += 1
            results = []
            for out, ref in zip(out_shapes, outputs):
                if len(out) > 2:
                    target = out[4](ref) if len(out) > 3 else ref
                    results.append(Send(held.pop(0), target, [sems.at[used + index] for index in range(4)]))
                    used += 4
                else:
                    results.append(ref)
            assert used <= sem_count
            given = [item() if kind == "f" else item for kind, item in zip(plan, given)]
            body(*given, *results, *rest)
            for item in given:
                if isinstance(item, Fetch):
                    item()
            sends = [item for item in results if isinstance(item, Send)]
            for item in sends:
                item.finish()
            for item in sends:
                for copy in item.copies:
                    copy.wait()

        return pl.pallas_call(
            outer,
            out_shape=[jax.ShapeDtypeStruct(out[0], out[1]) for out in out_shapes],
            in_specs=in_specs,
            out_specs=[pl.BlockSpec(memory_space=pl.ANY if len(out) > 2 else pltpu.VMEM) for out in out_shapes],
            scratch_shapes=buffers
            + [pltpu.SemaphoreType.DMA((sem_count,))]
            + [pltpu.VMEM(shape, kind) for shape, kind in scratch]
            + extra,
            input_output_aliases=aliases or {},
            compiler_params=pltpu.CompilerParams(vmem_limit_bytes=megas * MEGA),
            cost_estimate=pl.CostEstimate(flops=0, bytes_accessed=0, transcendentals=0),
        )(*operands)

    return call


def fill_bounds(lengths_ref, bounds_s, total):
    bounds_s[0] = jnp.int32(0)
    end = jnp.int32(0)
    for item in range(ITEMS):
        end = end + lengths_ref[0, item]
        bounds_s[item + 1] = end
    for item in range(ITEMS + 1, BOUNDS):
        bounds_s[item] = jnp.int32(total)


def select_kernel(
    up_ref,
    up_bias_ref,
    gain_ref,
    bias_ref,
    conv_bias_ref,
    taps_ref,
    qkv_ref,
    pos_ref,
    content_ref,
    position_ref,
    up_out,
    table_out,
    qkv_out,
    pos_out,
    bias_out,
):
    place = lax.axis_index("tm")
    quarters = lax.axis_size("stream")
    share = HALF // (quarters * lax.axis_size("tm"))
    lane = lax.broadcasted_iota(jnp.int32, (1, 2 * LANES), 1)
    channel = jnp.where(lane < LANES + LOW, lane, lane - LOW)
    group = jnp.zeros_like(channel)
    for quarter in range(1, quarters):
        group = group + (channel >= quarter * share).astype(jnp.int32)
    source = group * (HALF // quarters) + share * place + channel - group * share
    chosen = (lax.broadcasted_iota(jnp.int32, (HALF, 2 * LANES), 0) == source).astype(F32).astype(BF16)
    gate = dot_nn(up_ref[:, :HALF], chosen)
    conv = dot_nn(up_ref[:, HALF:], chosen)
    up_out[:, :LANES] = gate[:, :LANES].astype(BF16)
    up_out[:, LANES : 2 * LANES] = jnp.where(low_lanes(D), gate[:, LANES:], conv[:, LANES:]).astype(BF16)
    up_out[:, 2 * LANES :] = conv[:, :LANES].astype(BF16)
    up_bias = line_of(up_bias_ref)
    lines = jnp.concatenate(
        [
            up_bias[:, :HALF],
            up_bias[:, HALF:],
            line_of(gain_ref),
            line_of(bias_ref),
            line_of(conv_bias_ref),
            jnp.zeros((3, HALF), F32),
        ],
        axis=0,
    )
    lines = dot_nn(lines.astype(BF16), chosen)
    taps = dot_nn(taps_ref[...], chosen)
    for part in range(2):
        lanes = slice(part * LANES, (part + 1) * LANES)
        table_out[part, :8] = lines[:, lanes]
        table_out[part, 8 : 8 + KERNEL] = taps[:, lanes]
        table_out[part, 8 + KERNEL :] = jnp.zeros((1, LANES), F32)

    odd = lax.rem(place, 2) == 1

    def head_lanes(ref, base):
        at = pl.ds(pl.multiple_of(lax.div(place, 2) * LANES + base, LANES), LANES)
        values = ref[:, at].astype(F32)
        values = jnp.where(odd, turn(values), values)
        return jnp.where(low_lanes(values.shape[0]), values, 0.0)

    for part in range(3):
        qkv_out[:, part * LANES : (part + 1) * LANES] = head_lanes(qkv_ref, part * D).astype(BF16)
    pos_out[...] = head_lanes(pos_ref, 0).astype(BF16)
    bias_out[...] = jnp.zeros((8, LANES), F32)
    for line, ref in enumerate((content_ref, position_ref)):
        values = line_of(ref)
        picked = values[:, :LANES]
        for tile in range(1, D // LANES):
            picked = jnp.where(
                lax.div(place, 2) == tile, values[:, tile * LANES : (tile + 1) * LANES], picked
            )
        picked = jnp.where(odd, turn(picked), picked)
        bias_out[line : line + 1] = jnp.where(low_lanes(1), picked, 0.0)


def angle_rows(coarse_ref, fine_ref, block, rows):
    half = D // 2
    base = coarse_ref[pl.ds(block, 1)]
    base_sine, base_cosine = base[:, :half], base[:, half:]
    sine, cosine = fine_ref[rows, :half], fine_ref[rows, half:]
    return base_sine * cosine + base_cosine * sine, base_cosine * cosine - base_sine * sine


def item_codes(bounds_s, index):
    code = jnp.zeros_like(index)
    for item in range(1, ITEMS + 1):
        code = code + (index >= bounds_s[item]).astype(jnp.int32)
    return jnp.where(code < ITEMS, code, ITEMS + index)


def attend_kernel(
    lengths_ref,
    x_ref,
    attn_gain_ref,
    attn_bias_ref,
    mlp_gain_ref,
    mlp_bias_ref,
    qkv_ref,
    pos_ref,
    bias_ref,
    coarse_ref,
    fine_ref,
    up_ref,
    up_bias_ref,
    n_attn_out,
    n_mlp_out,
    hat_out,
    q_position_out,
    query_out,
    key_out,
    value_out,
    prob_out,
    attn_out,
    stats_out,
    bounds_s,
):
    frames = n_attn_out.buffer.shape[0]
    half = D // 2
    fill_bounds(lengths_ref, bounds_s, frames)
    attn_gain, attn_bias = line_of(attn_gain_ref), line_of(attn_bias_ref)
    mlp_gain, mlp_bias = line_of(mlp_gain_ref), line_of(mlp_bias_ref)
    content, position = bias_ref[0:1], bias_ref[1:2]
    x_ref = x_ref()
    begin(up_ref)

    @pl.loop(0, frames // TALL, unroll=4)
    def _(block):
        rows = rows_of(block, TALL)
        for part in range(TALL // 32):
            at = pl.ds(pl.multiple_of(block * TALL + part * 32, 32), 32)
            hat = centre_rows(x_ref[at].astype(F32))
            hat_out.buffer[at] = hat.astype(BF16)
            n_attn_out.buffer[at] = (hat * attn_gain + attn_bias).astype(BF16)
            n_mlp_out.buffer[at] = (hat * mlp_gain + mlp_bias).astype(BF16)
        parts = dot_nn(n_attn_out.buffer[rows], qkv_ref[...])
        query = parts[:, :LANES]
        query_out.buffer[rows, :LANES] = ((query + content).astype(BF16).astype(F32) * 0.125).astype(BF16)
        q_position = (query + position).astype(BF16)
        q_position_out.buffer[rows] = q_position
        key_out.buffer[rows, :LANES] = parts[:, LANES : 2 * LANES].astype(BF16)
        value_out.buffer[rows] = parts[:, 2 * LANES :].astype(BF16)
        projected = dot_nt(q_position, pos_ref[...])
        for part in range(TALL // 32):
            at = pl.ds(pl.multiple_of(block * TALL + part * 32, 32), 32)
            inner = part * 32 % BLOCK
            sine, cosine = angle_rows(
                coarse_ref, fine_ref, block * (TALL // BLOCK) + part * 32 // BLOCK, slice(inner, inner + 32)
            )
            first = projected[part * 32 : part * 32 + 32, :half]
            second = projected[part * 32 : part * 32 + 32, half:]
            query_out.buffer[at, LANES : LANES + half] = ((first * sine + second * cosine) * 0.125).astype(BF16)
            query_out.buffer[at, LANES + half :] = ((second * sine - first * cosine) * 0.125).astype(BF16)
            key_out.buffer[at, LANES : LANES + half] = cosine.astype(BF16)
            key_out.buffer[at, LANES + half :] = sine.astype(BF16)

    for out in (n_attn_out, n_mlp_out, hat_out, q_position_out, query_out, key_out, value_out):
        out.go()
    up_ref = up_ref()
    up_bias = line_of(up_bias_ref)[:, HALF:]
    lane = lax.broadcasted_iota(jnp.int32, (16, LANES), 1)

    @pl.loop(0, frames // TALL, unroll=2)
    def _(block):
        values = dot_nn(n_mlp_out.buffer[rows_of(block, TALL)], up_ref[...])
        for part in range(TALL // 16):
            pre = values[part * 16 : part * 16 + 16] + up_bias
            hidden = pre * (0.5 + 0.5 * lax.erf(pre * math.sqrt(0.5)))
            mean = jnp.mean(hidden, axis=-1, keepdims=True)
            centred = hidden - mean
            rate = lax.rsqrt(jnp.mean(centred * centred, axis=-1, keepdims=True) + EPS)
            at = pl.ds(pl.multiple_of(block * TALL + part * 16, 16), 16)
            stats_out.buffer[at] = jnp.where(lane == 0, mean, rate)

    stats_out.go()
    key_code = item_codes(bounds_s, lax.broadcasted_iota(jnp.int32, (1, frames), 1))

    low = low_lanes(32)
    for block in range(frames // TALL):
        rows = pl.ds(block * TALL, TALL)
        raw = dot_nt(query_out.buffer[rows], key_out.buffer[...])
        shares = []
        for part in range(TALL // 32):
            start = block * TALL + part * 32
            index = start + lax.broadcasted_iota(jnp.int32, (32, 1), 0)
            scaled = jnp.where(
                item_codes(bounds_s, index) == key_code, raw[part * 32 : part * 32 + 32], MASKED
            )
            weight = jnp.exp(scaled - jnp.max(scaled, axis=1, keepdims=True))
            prob_out.buffer[pl.ds(start, 32)] = weight.astype(BF16)
            shares.append(1.0 / jnp.sum(weight, axis=1, keepdims=True))
        prob_out.go(rows)
        attn = dot_nn(prob_out.buffer[rows], value_out.buffer[...])
        for part in range(TALL // 32):
            share = shares[part]
            attn_out.buffer[pl.ds(block * TALL + part * 32, 32)] = jnp.where(
                low, attn[part * 32 : part * 32 + 32] * share, share
            )


def fill_margins(wide_s, frames):
    edge = jnp.zeros((MARGIN, LANES), F32)
    wide_s[:MARGIN] = edge
    wide_s[MARGIN + frames : 2 * MARGIN + frames] = edge
    base = frames + 3 * MARGIN
    after = base + frames // 2
    low = low_lanes(MARGIN)
    wide_s[base - MARGIN : base] = jnp.where(low, 0.0, turn(wide_s[after - MARGIN : after]))
    wide_s[after : after + MARGIN] = jnp.where(low, turn(wide_s[base : base + MARGIN]), 0.0)


def item_span(bounds_s, frame):
    begin, end = bounds_s[0], bounds_s[BOUNDS - 1]
    for item in range(1, ITEMS + 1):
        edge = bounds_s[item]
        begin = jnp.where(frame >= edge, edge, begin)
    for item in range(ITEMS, 0, -1):
        edge = bounds_s[item]
        end = jnp.where(frame < edge, edge, end)
    return begin, end


def is_whole(bounds_s, start):
    begin, end = item_span(bounds_s, start)
    reach = KERNEL // 2
    low = (begin == 0) | (begin <= start - reach)
    high = (end == bounds_s[BOUNDS - 1]) | (end >= start + WINDOW + reach)
    return low & high & (end >= start + WINDOW)


def tap_limits(bounds_s, start):
    frame = start + lax.broadcasted_iota(jnp.int32, (WINDOW, LANES), 0)
    begin, end = item_span(bounds_s, frame)
    return begin - frame, end - frame


def grouped(values):
    return values.reshape(WINDOW // 8, 8, LANES)


def triple_places(step, frames):
    half = frames // 2
    return (
        pl.multiple_of(step * WINDOW, 2 * MARGIN),
        pl.multiple_of(step * WINDOW + half, 2 * MARGIN),
        pl.multiple_of(step * WINDOW + frames + 2 * MARGIN, 2 * MARGIN),
    )


def over_windows(bounds_s, frames, body):
    half = frames // 2

    @pl.loop(0, half // WINDOW)
    def _(step):
        start = step * WINDOW
        whole = is_whole(bounds_s, start) & is_whole(bounds_s, start + half)

        @pl.when(whole)
        def _():
            body(step, None)

        @pl.when(jnp.logical_not(whole))
        def _():
            first, second = tap_limits(bounds_s, start), tap_limits(bounds_s, start + half)
            low = low_lanes(WINDOW)
            rest = [jnp.where(low, one, other) for one, other in zip(first, second)]
            body(step, (first, second, rest))


def tap_mask(tap, limits):
    shift = tap - KERNEL // 2
    return None if limits is None else (limits[0] <= shift) & (limits[1] > shift)


def tap_view(window_ref, tap, mask):
    view = window_ref[tap + 1 : tap + 1 + WINDOW]
    return grouped(view if mask is None else jnp.where(mask, view, 0.0))


def mlp_first_kernel(
    lengths_ref,
    n_ref,
    up_ref,
    table_ref,
    stats_ref,
    cot_ref,
    merge_ref,
    down_ref,
    attn_ref,
    mixed_out,
    gate_pre_out,
    grad_out,
    rate_out,
    hat_out,
    early_out,
    vectors_out,
    lines_out,
    hat_s,
    slope_s,
    gate_s,
    hidden_s,
    gate_slope_s,
    conv_s,
    grad_s,
    out_s,
    back_s,
    branch_s,
    mix_s,
    taps_s,
    turn_s,
    tap_sum_s,
    columns_s,
    forward_s,
    backward_s,
    bounds_s,
):
    place = lax.axis_index("tm")
    frames = mix_s.shape[0]
    half = frames // 2
    blocks = frames // BLOCK
    quarters, early_rows, _ = early_out.buffer.shape
    share = early_rows // 8
    channels = quarters * share
    fill_bounds(lengths_ref, bounds_s, frames)
    for part in range(2):
        for tap in range(KERNEL):
            line = jnp.broadcast_to(table_ref[part, 8 + tap : 9 + tap], (8, LANES))
            taps_s[part, tap] = line
            turn_s[part, KERNEL - 1 - tap] = line
    tap_sum_s[...] = jnp.zeros(tap_sum_s.shape, F32)
    main, rest = table_ref[0, :8], table_ref[1, :8]
    mixed_bias = jnp.where(low_lanes(1), rest[0:1], rest[1:2])
    low = low_lanes(64)
    gate_pre_ref = gate_pre_out.buffer
    n_ref = n_ref()
    stats_ref = stats_ref()
    begin(cot_ref, merge_ref, down_ref, attn_ref)

    def stat_rows(rows):
        stats = stats_ref[rows]
        return stats[:, 0:1], stats[:, 1:2]

    def chunk(start, base=0):
        return pl.ds(pl.multiple_of(start, 64) + base, 64)

    def conv_part(hidden, mean, rate, lines, rows, to_rows):
        hat = (hidden - mean) * rate
        hat_s[rows] = hat
        hat_out.buffer[rows] = hat.astype(BF16)
        conv_s[to_rows] = (hat * lines[2:3] + lines[3:4]).astype(BF16).astype(F32)

    @pl.loop(0, half // TALL, unroll=2)
    def _(block):
        pre = [dot_nn(n_ref[rows_of(block, TALL, base)], up_ref[...]) for base in (0, half)]
        for part in range(TALL // 64):
            inner = slice(part * 64, part * 64 + 64)
            start = block * TALL + part * 64
            mixed = []
            for values, base in zip(pre, (0, half)):
                rows = chunk(start, base)
                gate, gate_slope = gelu_parts(values[inner, :LANES] + main[0:1])
                hidden_s[rows] = gate
                gate_slope_s[rows] = gate_slope
                hidden, slope = gelu_parts(values[inner, 2 * LANES :] + main[1:2])
                mean, rate = stat_rows(rows)
                slope_s[rows] = slope * rate
                conv_part(hidden, mean, rate, main, rows, chunk(start, base + MARGIN))
                mixed.append((*gelu_parts(values[inner, LANES : 2 * LANES] + mixed_bias), mean, rate))
            (low_hidden, low_slope, low_mean, low_rate), (high_hidden, high_slope, high_mean, high_rate) = mixed
            rows = chunk(start, frames)
            hidden_s[rows] = jnp.where(low, low_hidden, turn(high_hidden))
            gate_slope_s[rows] = jnp.where(low, low_slope, turn(high_slope))
            rate = jnp.where(low, low_rate, high_rate)
            slope_s[rows] = jnp.where(low, turn(low_slope), high_slope) * rate
            conv_part(
                jnp.where(low, turn(low_hidden), high_hidden),
                jnp.where(low, low_mean, high_mean),
                rate,
                rest,
                rows,
                chunk(start, frames + 3 * MARGIN),
            )

    hat_out.go()
    fill_margins(conv_s, frames)
    tall = WINDOW + 2 * MARGIN
    outs = (0, half, frames)

    def convolve(step, limits):
        for index, base in enumerate(triple_places(step, frames)):
            forward_s[index] = conv_s[pl.ds(base, tall)]
        for index in range(3):
            own = None if limits is None else limits[index]
            total = jnp.zeros((WINDOW // 8, 8, LANES), F32)
            for tap in range(KERNEL):
                mask = tap_mask(tap, own)
                total = total + tap_view(forward_s.at[index], tap, mask) * taps_s[index // 2, tap][None]
            lines = rest if index == 2 else main
            out_s[rows_of(step, WINDOW, outs[index])] = total.reshape(WINDOW, LANES) + lines[4:5]

    over_windows(bounds_s, frames, convolve)
    cot_ref = cot_ref()
    merge_ref = merge_ref()
    down_ref = down_ref()
    attn_ref = attn_ref()
    down_ref[channels:] = jnp.zeros((2 * LANES - channels, D), BF16)
    zero = jnp.zeros((8, LANES), F32)

    def branch_part(grad_gated, rows, to_rows, sums):
        up_sum, conv_sum = sums
        gate, conv = hidden_s[rows], out_s[rows]
        gate_pre = (grad_gated * conv * gate_slope_s[rows]).astype(BF16)
        gate_pre_ref[rows] = gate_pre
        grad_conv = (grad_gated * gate).astype(BF16).astype(F32)
        grad_s[to_rows] = grad_conv
        gate_pre = gate_pre.astype(F32)
        return gate * conv, gate_pre, (up_sum + fold_rows(gate_pre), conv_sum + fold_rows(grad_conv))

    def branch_step(block, sums):
        main_sums, rest_sums = sums
        grads = []
        for base in (0, half):
            rows = rows_of(block, TALL, base)
            branch = dot_nt(cot_ref[rows], merge_ref[...]).astype(BF16)
            branch_s[rows] = branch
            grads.append(dot_nt(branch, down_ref[...]))
        for part in range(TALL // 64):
            inner = slice(part * 64, part * 64 + 64)
            start = block * TALL + part * 64
            for values, base in zip(grads, (0, half)):
                rows = chunk(start, base)
                gated, gate_pre, main_sums = branch_part(
                    values[inner, :LANES], rows, chunk(start, base + MARGIN), main_sums
                )
                mix_s[rows, :LANES] = gated.astype(BF16)
                gate_s[rows, :LANES] = gate_pre.astype(BF16)
            grad = jnp.where(low, grads[0][inner, LANES:], turn(grads[1][inner, LANES:]))
            gated, gate_pre, rest_sums = branch_part(
                grad, chunk(start, frames), chunk(start, frames + 3 * MARGIN), rest_sums
            )
            low_rows, high_rows = chunk(start), chunk(start, half)
            gate_s[low_rows, LANES:] = gate_pre.astype(BF16)
            gate_s[high_rows, LANES:] = turn(gate_pre).astype(BF16)
            mix_s[low_rows, LANES:] = jnp.where(low, gated, turn(attn_ref[low_rows])).astype(BF16)
            mix_s[high_rows, LANES:] = jnp.where(low, turn(gated), turn(attn_ref[high_rows])).astype(BF16)
        return main_sums, rest_sums

    (main_up, main_conv), (rest_up, rest_conv) = lax.fori_loop(
        0, half // TALL, branch_step, ((zero, zero), (zero, zero)), unroll=2
    )
    gate_pre_out.go()
    fill_margins(grad_s, frames)
    own = rows_of(place, BLOCK)
    lines_out[0:1] = one_row(fold_rows(branch_s[own].astype(F32)))
    lines_out[1:2] = one_row(fold_rows(cot_ref[own].astype(F32)))
    lines_out[2:8] = jnp.zeros((6, D), F32)
    grad_down = dot_tn(mix_s[...], branch_s[...])
    grad_gate = dot_tn(gate_s[...], n_ref[...])
    for quarter in range(quarters):
        for tile in range(4):
            early_out.buffer[quarter, tile * share : (tile + 1) * share] = grad_down[
                quarter * share : (quarter + 1) * share, tile * LANES : (tile + 1) * LANES
            ].astype(BF16)
        early_out.buffer[quarter, 4 * share :] = grad_gate[
            :channels, quarter * LANES : (quarter + 1) * LANES
        ].astype(BF16)
    early_out.go()
    for block in range(blocks):
        mixed_out.buffer[block, :BLOCK] = mix_s[block * BLOCK : (block + 1) * BLOCK]
    mixed_out.go(slice(None), pl.ds(0, BLOCK))

    def differentiate(step, limits):
        for index, base in enumerate(triple_places(step, frames)):
            forward_s[index] = conv_s[pl.ds(base, tall)]
            backward_s[index] = grad_s[pl.ds(base, tall)]
        for index in range(3):
            own = None if limits is None else limits[index]
            total = jnp.zeros((WINDOW // 8, 8, LANES), F32)
            centre = grouped(backward_s[index, MARGIN : MARGIN + WINDOW])
            for tap in range(KERNEL):
                mask = tap_mask(tap, own)
                total = total + tap_view(backward_s.at[index], tap, mask) * turn_s[index // 2, tap][None]
                tap_sum_s[index // 2, tap] += jnp.sum(tap_view(forward_s.at[index], tap, mask) * centre, axis=0)
            back_s[rows_of(step, WINDOW, outs[index])] = total.reshape(WINDOW, LANES)

    over_windows(bounds_s, frames, differentiate)
    lane = lax.broadcasted_iota(jnp.int32, (64, LANES), 1)

    def norm_part(rows, lines, sums):
        gain_sum, bias_sum = sums
        back, hat, slope = back_s[rows], hat_s[rows], slope_s[rows]
        grad = back * lines[2:3]
        grad_out.buffer[rows] = (grad * slope).astype(BF16)
        rate_out.buffer[rows] = slope.astype(BF16)
        along = back * hat
        return grad, along * lines[2:3], (gain_sum + fold_rows(along), bias_sum + fold_rows(back))

    def norm_step(block, sums):
        main_sums, rest_sums = sums
        for part in range(TALL // 64):
            start = block * TALL + part * 64
            pairs = []
            for base in (0, half):
                plain, along, main_sums = norm_part(chunk(start, base), main, main_sums)
                pairs.append([plain, along])
            plain, along, rest_sums = norm_part(chunk(start, frames), rest, rest_sums)
            for item, values in enumerate((plain, along)):
                pairs[0][item] = pairs[0][item] + jnp.where(low, values, 0.0)
                pairs[1][item] = pairs[1][item] + jnp.where(low, 0.0, values)
            for (plain, along), base in zip(pairs, (0, half)):
                columns_s[chunk(start, base)] = jnp.where(
                    lane == 0,
                    jnp.sum(plain, axis=-1, keepdims=True),
                    jnp.where(lane == 1, jnp.sum(along, axis=-1, keepdims=True), 0.0),
                )
        return main_sums, rest_sums

    (main_gain, main_bias), (rest_gain, rest_bias) = lax.fori_loop(
        0, half // TALL, norm_step, ((zero, zero), (zero, zero)), unroll=2
    )
    grad_out.go()
    rate_out.go()
    totals = jnp.concatenate(
        [jnp.transpose(columns_s[block * BLOCK : (block + 1) * BLOCK])[:2] for block in range(blocks)], axis=0
    )
    high = totals.astype(BF16)
    low_part = (totals - high.astype(F32)).astype(BF16)
    for block in range(blocks):
        mixed_out.buffer[block, BLOCK:, :LANES] = high
        mixed_out.buffer[block, BLOCK:, LANES:] = low_part
    mixed_out.go(slice(None), pl.ds(BLOCK, 2 * blocks))

    def vectors(part, lines):
        taps = jnp.sum(tap_sum_s[part], axis=1)[:KERNEL]
        stacked = jnp.concatenate([taps] + [one_row(line) for line in lines], axis=0)
        if part:
            stacked = stacked + turn(stacked)
        return jnp.transpose(
            jnp.concatenate([stacked, jnp.zeros((LANES - stacked.shape[0], LANES), F32)], axis=0)
        )

    vectors_out[:LANES] = vectors(0, (main_conv, main_gain, main_bias, main_up))
    vectors_out[LANES:] = vectors(1, (rest_conv, rest_gain, rest_bias, rest_up))[: channels - LANES]


def attend_back_kernel(
    cot_ref,
    merge_ref,
    head_ref,
    attn_ref,
    value_ref,
    prob_ref,
    key_ref,
    coarse_ref,
    fine_ref,
    pos_ref,
    query_ref,
    n_ref,
    q_position_ref,
    qkv_ref,
    hat_ref,
    gain_ref,
    early_ref,
    branch_out,
    total_out,
    pack_0,
    pack_1,
    pack_2,
    pack_3,
    lines_out,
    grad_s,
    raw_s,
    projected_s,
    parts_s,
    grads_s,
):
    place = lax.axis_index("tm")
    frames = raw_s.shape[0]
    blocks = frames // BLOCK
    half = D // 2
    zero = jnp.zeros((8, LANES), F32)
    cot_ref, merge_ref, head_ref, attn_ref = cot_ref(), merge_ref(), head_ref(), attn_ref()
    head_ref[HEAD:] = jnp.zeros((LANES - HEAD, D), BF16)
    begin(value_ref, prob_ref, key_ref, pos_ref)

    @pl.loop(0, frames // TALL, unroll=4)
    def _(block):
        rows = rows_of(block, TALL)
        branch = dot_nt(cot_ref[rows], merge_ref[...]).astype(BF16)
        branch_out.buffer[rows] = branch
        grad_s[rows] = (dot_nt(branch, head_ref[...]) * attn_ref[rows, HEAD : HEAD + 1]).astype(BF16)

    branch_out.go()
    value_ref, prob_ref = value_ref(), prob_ref()
    key_ref, pos_ref = key_ref(), pos_ref()
    begin(query_ref, n_ref, q_position_ref, qkv_ref, hat_ref, early_ref)

    def score_step(block, sums):
        content_sum, position_sum = sums
        rows = rows_of(block, TALL)
        grad = grad_s[rows]
        score = dot_nt(grad, value_ref[...])
        for part in range(TALL // 32):
            at = pl.ds(pl.multiple_of(block * TALL + part * 32, 32), 32)
            inner = slice(part * 32, part * 32 + 32)
            delta = jnp.sum(grad[inner].astype(F32) * attn_ref[at], axis=1, keepdims=True)
            raw_s[at] = (prob_ref[at].astype(F32) * (score[inner] - delta)).astype(BF16)
        query = dot_nn(raw_s[rows], key_ref[...]) * 0.125
        for part in range(TALL // 32):
            at = pl.ds(pl.multiple_of(block * TALL + part * 32, 32), 32)
            inner = part * 32 % BLOCK
            sine, cosine = angle_rows(
                coarse_ref, fine_ref, block * (TALL // BLOCK) + part * 32 // BLOCK, slice(inner, inner + 32)
            )
            inner = slice(part * 32, part * 32 + 32)
            first, second = query[inner, LANES : LANES + half], query[inner, LANES + half :]
            projected_s[at, :half] = (first * sine - second * cosine).astype(BF16)
            projected_s[at, half:] = (first * cosine + second * sine).astype(BF16)
        position = dot_nn(projected_s[rows], pos_ref[...])
        content = query[:, :LANES]
        parts_s[rows, :LANES] = (content + position).astype(BF16)
        return content_sum + fold_rows(content), position_sum + fold_rows(position)

    content_sum, position_sum = lax.fori_loop(0, frames // TALL, score_step, (zero, zero), unroll=4)
    query_ref, n_ref, q_position_ref = query_ref(), n_ref(), q_position_ref()
    qkv_ref, hat_ref = qkv_ref(), hat_ref()
    grad_key = dot_tn(query_ref[...], raw_s[...])
    grad_value = dot_tn(grad_s[...], prob_ref[...])
    for block in range(blocks):
        at = slice(block * BLOCK, (block + 1) * BLOCK)
        parts_s[at, LANES : 2 * LANES] = jnp.transpose(grad_key[:, at]).astype(BF16)
        parts_s[at, 2 * LANES :] = jnp.transpose(grad_value[:, at]).astype(BF16)
    grads_s[:HEAD] = dot_tn(parts_s[:, :LANES], n_ref[...])[:HEAD]
    grads_s[HEAD : 2 * HEAD] = dot_nn(grad_key.astype(BF16), n_ref[...])[:HEAD]
    grads_s[2 * HEAD : 3 * HEAD] = dot_nn(grad_value.astype(BF16), n_ref[...])[:HEAD]
    grads_s[3 * HEAD :] = dot_tn(q_position_ref[...], projected_s[...])[:HEAD]
    stream = lax.axis_index("stream")
    early_ref = early_ref()
    for apart, pack_out in enumerate((pack_0, pack_1, pack_2, pack_3)):
        quarter = lax.bitwise_xor(stream, jnp.int32(apart))
        lanes = pl.ds(pl.multiple_of(quarter * LANES, LANES), LANES)
        pack_out.buffer[: 4 * HEAD] = grads_s[:, lanes].astype(BF16)
        pack_out.buffer[4 * HEAD :] = early_ref[quarter]
        pack_out.go()
    gain = line_of(gain_ref)
    wide_zero = jnp.zeros((8, D), F32)

    def norm_step(block, sums):
        gain_sum, bias_sum = sums
        grad = dot_nt(parts_s[rows_of(block, TALL)], qkv_ref[...])
        for part in range(TALL // 32):
            at = pl.ds(pl.multiple_of(block * TALL + part * 32, 32), 32)
            own = grad[part * 32 : part * 32 + 32]
            total_out.buffer[at] = (own * gain).astype(BF16)
            gain_sum = gain_sum + fold_rows(own * hat_ref[at].astype(F32))
            bias_sum = bias_sum + fold_rows(own)
        return gain_sum, bias_sum

    gain_sum, bias_sum = lax.fori_loop(0, frames // TALL, norm_step, (wide_zero, wide_zero), unroll=4)
    lane = lax.broadcasted_iota(jnp.int32, (1, LANES), 1)

    def own_lanes(sums):
        line = one_row(sums)
        line = line + turn(line)
        tiles = [
            jnp.where(lax.div(tile * LANES + lane, HEAD) == place, line, 0.0) for tile in range(D // LANES)
        ]
        return jnp.concatenate(tiles, axis=1)

    lines_out[...] = jnp.concatenate(
        [
            one_row(gain_sum),
            one_row(bias_sum),
            own_lanes(content_sum),
            own_lanes(position_sum),
            jnp.zeros((4, D), F32),
        ],
        axis=0,
    )


def mlp_second_kernel(
    mixed_ref,
    gate_pre_ref,
    grad_ref,
    rate_ref,
    hat_ref,
    up_ref,
    norm_hat_ref,
    gain_ref,
    other_ref,
    pre_out,
    same_out,
    apart_out,
    lines_out,
    up_out,
    columns_s,
):
    place = lax.axis_index("tm")
    pre_s = pre_out.buffer
    frames = pre_s.shape[0]
    half = frames // 2
    blocks = frames // BLOCK
    totals = jnp.zeros((2 * blocks, LANES), F32)
    mixed_ref = mixed_ref()
    for source in range(mixed_ref.shape[0]):
        both = mixed_ref[source].astype(F32)
        totals = totals + (both[:, :LANES] + both[:, LANES:])
    totals = totals * (1.0 / HALF)
    columns = jnp.transpose(jnp.concatenate([totals, jnp.zeros((LANES - 2 * blocks, LANES), F32)], axis=0))
    lane = lax.broadcasted_iota(jnp.int32, (BLOCK, LANES), 1)
    for block in range(blocks):
        columns_s[block * BLOCK : (block + 1) * BLOCK] = jnp.where(
            lane == 0, columns[:, 2 * block : 2 * block + 1], columns[:, 2 * block + 1 : 2 * block + 2]
        )
    gate_pre_ref, grad_ref, rate_ref, hat_ref = gate_pre_ref(), grad_ref(), rate_ref(), hat_ref()
    begin(up_ref, norm_hat_ref, other_ref)
    low = low_lanes(64)
    gain = line_of(gain_ref)

    def chunk(start, base=0):
        return pl.ds(pl.multiple_of(start, 64) + base, 64)

    def pre_part(rows, table, up_sum):
        plain, along = table
        hat, rate = hat_ref[rows].astype(F32), rate_ref[rows].astype(F32)
        pre = (grad_ref[rows].astype(F32) - rate * (plain + hat * along)).astype(BF16).astype(F32)
        return pre, up_sum + fold_rows(pre)

    def pre_step(block, sums):
        main_up, rest_up = sums
        for part in range(TALL // 64):
            start = block * TALL + part * 64
            tables = []
            for base in (0, half):
                rows = chunk(start, base)
                values = columns_s[rows]
                table = [values[:, item : item + 1] for item in range(2)]
                tables.append(table)
                pre, main_up = pre_part(rows, table, main_up)
                pre_s[rows, :LANES] = gate_pre_ref[rows]
                pre_s[rows, 2 * LANES :] = pre.astype(BF16)
            rows = chunk(start, frames)
            table = [jnp.where(low, one, other) for one, other in zip(*tables)]
            pre, rest_up = pre_part(rows, table, rest_up)
            gate_pre = gate_pre_ref[rows].astype(F32)
            pre_s[chunk(start), LANES : 2 * LANES] = jnp.where(low, gate_pre, turn(pre)).astype(BF16)
            pre_s[chunk(start, half), LANES : 2 * LANES] = jnp.where(low, turn(gate_pre), pre).astype(BF16)
        return main_up, rest_up

    zero = jnp.zeros((8, LANES), F32)
    main_up, rest_up = lax.fori_loop(0, half // TALL, pre_step, (zero, zero), unroll=2)
    pre_out.go()
    up_ref, norm_hat_ref, other_ref = up_ref(), norm_hat_ref(), other_ref()
    wide_zero = jnp.zeros((8, D), F32)

    def norm_step(step, sums):
        gain_sum, bias_sum = sums
        grads = dot_nt(pre_s[rows_of(step, TALL)], up_ref[...])
        for part in range(TALL // BLOCK):
            block = step * (TALL // BLOCK) + part
            rows = rows_of(block, BLOCK)
            grad = grads[part * BLOCK : (part + 1) * BLOCK]
            total = (grad * gain + other_ref[rows].astype(F32)).astype(BF16)
            apart = lax.bitwise_xor(block, place)

            @pl.when(lax.rem(apart, 2) == 0)
            def _(apart=apart, total=total):
                same_out.buffer[lax.div(apart, 2)] = total

            @pl.when(lax.rem(apart, 2) == 1)
            def _(apart=apart, total=total):
                apart_out.buffer[lax.div(apart, 2)] = total

            gain_sum = gain_sum + fold_rows(grad * norm_hat_ref[rows].astype(F32))
            bias_sum = bias_sum + fold_rows(grad)
        return gain_sum, bias_sum

    gain_sum, bias_sum = lax.fori_loop(0, frames // TALL, norm_step, (wide_zero, wide_zero), unroll=2)
    apart_out.go()
    same_out.go()
    lines_out[...] = jnp.concatenate([one_row(gain_sum), one_row(bias_sum), jnp.zeros((6, D), F32)], axis=0)
    rest_line = one_row(rest_up)
    up_out[:LANES] = jnp.transpose(jnp.broadcast_to(one_row(main_up), (LANES, LANES)))
    up_out[LANES:] = jnp.transpose(jnp.broadcast_to(rest_line + turn(rest_line), (LANES, LANES)))[:LOW]


def late_pack_kernel(
    pre_ref,
    n_ref,
    joined_ref,
    branch_ref,
    cot_ref,
    vectors_ref,
    up_columns_ref,
    first_lines_ref,
    head_lines_ref,
    own_lines_ref,
    pack_out,
):
    pack_ref = pack_out.buffer
    quarters = pack_ref.shape[0]
    channels = vectors_ref.shape[0]
    share = channels // quarters
    gate_at = KERNEL + 3
    lane = lax.broadcasted_iota(jnp.int32, (share, LANES), 1)
    lines = jnp.concatenate(
        [
            head_lines_ref[0:2],
            own_lines_ref[0:2],
            head_lines_ref[2:4],
            first_lines_ref[0:2],
            jnp.zeros((8, D), F32),
        ],
        axis=0,
    )
    for quarter in range(quarters):
        table = vectors_ref[quarter * share : (quarter + 1) * share]
        for other in range(2):
            at = slice((2 * (quarter % 2) + other) * share, (2 * (quarter % 2) + other + 1) * share)
            column = vectors_ref[at, gate_at : gate_at + 1] if quarter < quarters // 2 else up_columns_ref[at, 0:1]
            table = jnp.where(lane == gate_at + other, column, table)
        pack_ref[quarter, channels : channels + share] = table.astype(BF16)
        pack_ref[quarter, channels + share : channels + share + 16] = lines[
            :, quarter * LANES : (quarter + 1) * LANES
        ].astype(BF16)
    grad_up = dot_tn(pre_ref()[...], n_ref()[...])
    for quarter in range(quarters):
        lanes = slice(quarter * LANES, (quarter + 1) * LANES)
        pack_ref[quarter, :LANES] = grad_up[LANES:, lanes].astype(BF16)
        pack_ref[quarter, LANES:channels] = grad_up[LOW:LANES, lanes].astype(BF16)
    joined_ref, cot_ref, branch_ref = joined_ref(), cot_ref(), branch_ref()
    sources, _, rows = joined_ref.shape
    merge_rows = 2 * D // sources
    head_rows = D // sources
    grad_merge = jnp.zeros((merge_rows, D), F32)
    grad_head = jnp.zeros((head_rows, D), F32)
    for source in range(sources):
        at = slice(source * rows, (source + 1) * rows)
        joined = joined_ref[source]
        grad_merge = grad_merge + dot_nn(joined[:merge_rows], cot_ref[at])
        grad_head = grad_head + dot_nn(joined[merge_rows : merge_rows + head_rows], branch_ref[at])
    for quarter in range(quarters):
        base = channels + share + 16
        for grad in (grad_merge, grad_head):
            part = grad.shape[0] // quarters
            for tile in range(4):
                pack_ref[quarter, base : base + part] = grad[
                    quarter * part : (quarter + 1) * part, tile * LANES : (tile + 1) * LANES
                ].astype(BF16)
                base += part


def output_kernel(
    x_ref, mixed_ref, head_ref, down_ref, down_bias_ref, merge_ref, merge_bias_ref, out_ref, joined_out
):
    sources = mixed_ref.shape[0]
    rows = x_ref.shape[0]
    channels = HALF // sources
    share = channels // 4
    attn_parts = []
    branch_attn = jnp.zeros((rows, D), F32)
    branch_mlp = jnp.zeros((rows, D), F32)
    for source in range(sources):
        attn = turn(mixed_ref[source, :rows, LANES:].astype(F32))[:, :HEAD].astype(BF16)
        attn_parts.append(attn)
        branch_attn = branch_attn + dot_nn(attn, head_ref[source * HEAD : (source + 1) * HEAD])
        down = jnp.concatenate(
            [down_ref[(part * sources + source) * share : (part * sources + source + 1) * share] for part in range(4)],
            axis=0,
        )
        branch_mlp = branch_mlp + dot_nn(mixed_ref[source, :rows, :channels], down)
    joined = jnp.concatenate(
        [branch_attn.astype(BF16), (branch_mlp + line_of(down_bias_ref)).astype(BF16)], axis=1
    )
    result = x_ref[...].astype(F32) + dot_nn(joined, merge_ref[...]) + line_of(merge_bias_ref)
    out_ref[...] = result.astype(BF16)
    turned = jnp.transpose(joined.astype(F32))
    heads = jnp.transpose(jnp.concatenate(attn_parts, axis=1).astype(F32))
    merge_share = turned.shape[0] // (4 * sources)
    head_share = heads.shape[0] // (4 * sources)
    used = 4 * (merge_share + head_share)
    for target in range(sources):
        for part in range(4):
            at = (part * sources + target) * merge_share
            joined_out[target, part * merge_share : (part + 1) * merge_share] = turned[
                at : at + merge_share
            ].astype(BF16)
            at = (part * sources + target) * head_share
            to = 4 * merge_share + part * head_share
            joined_out[target, to : to + head_share] = heads[at : at + head_share].astype(BF16)
        joined_out[target, used:] = jnp.zeros((joined_out.shape[1] - used, rows), BF16)


def pair_kernel(same_ref, other_ref, *out_refs):
    for slot, out_ref in enumerate(out_refs):
        out_ref[...] = (same_ref[slot].astype(F32) + other_ref[slot].astype(F32)).astype(BF16)


def frames_kernel(x_ref, cot_ref, *refs):
    total_refs, out_ref = refs[:-1], refs[-1]
    for part in range(x_ref.shape[0] // 32):
        rows = slice(part * 32, part * 32 + 32)
        inputs = x_ref[rows].astype(F32)
        mean = jnp.mean(inputs, axis=-1, keepdims=True)
        centred = inputs - mean
        rate = lax.rsqrt(jnp.mean(centred * centred, axis=-1, keepdims=True) + EPS)
        hat = centred * rate
        grad = total_refs[0][rows].astype(F32)
        for total_ref in total_refs[1:]:
            grad = grad + total_ref[rows].astype(F32)
        plain = jnp.mean(grad, axis=-1, keepdims=True)
        along = jnp.mean(grad * hat, axis=-1, keepdims=True)
        out_ref[rows] = cot_ref[rows].astype(F32) + rate * (grad - plain - hat * along)


def add_kernel(*refs):
    out_ref = refs[-1]
    first = 0
    for at in range(0, len(refs) - 1, 4):
        total = refs[at][...].astype(F32)
        for ref in refs[at + 1 : at + 4]:
            total = total + ref[...].astype(F32)
        out_ref[first : first + total.shape[0]] = total.astype(BF16)
        first += total.shape[0]


def gather_parts(near_ref, far_ref, all_s):
    place = lax.axis_index("tm")
    for apart in range(all_s.shape[0]):
        part_ref = far_ref if apart % 2 else near_ref
        all_s[lax.bitwise_xor(jnp.int32(apart), place)] = part_ref[apart // 2]


def lines_from(all_s, base, size):
    return jnp.concatenate([all_s[source, base : base + size] for source in range(all_s.shape[0])], axis=0).astype(F32)


def add_streams_kernel(parts_ref, out_ref):
    total = parts_ref[0].astype(F32)
    for source in range(1, parts_ref.shape[0]):
        total = total + parts_ref[source].astype(F32)
    out_ref[...] = total.astype(BF16)


def early_kernel(near_ref, far_ref, qkv_out, pos_out, down_out, up_out, all_s):
    gather_parts(near_ref, far_ref, all_s)
    sources = all_s.shape[0]
    share = HALF // (4 * sources)
    for kind in range(4):
        lines = jnp.transpose(lines_from(all_s, kind * HEAD, HEAD))
        if kind < 3:
            qkv_out[:, kind * D : (kind + 1) * D] = lines
        else:
            pos_out[...] = lines
    base = 4 * HEAD
    for source in range(sources):
        for tile in range(4):
            down_out[source * share : (source + 1) * share, tile * LANES : (tile + 1) * LANES] = all_s[
                source, base + tile * share : base + (tile + 1) * share
            ].astype(F32)
    wide = sources * share
    for group in range(4):
        up_out.buffer[:, group * wide : (group + 1) * wide] = jnp.transpose(
            lines_from(all_s, base + 4 * share + group * share, share)
        )


def late_kernel(*refs):
    _, near_ref, far_ref = refs[:3]
    (
        attn_gain_out,
        attn_bias_out,
        mlp_gain_out,
        mlp_bias_out,
        content_out,
        position_out,
        outw_out,
        up_out,
        up_bias_out,
        gain_out,
        bias_out,
        taps_out,
        conv_bias_out,
        down_bias_out,
        merge_out,
        merge_bias_out,
        all_s,
    ) = refs[3:]
    gather_parts(near_ref, far_ref, all_s)
    sources = all_s.shape[0]
    channels = HALF // sources
    share = channels // 4
    base = 0
    for group in range(4):
        at = group * sources * share
        up_out.buffer[:, at : at + sources * share] = jnp.transpose(lines_from(all_s, base + group * share, share))
    up_out.go()
    table = jnp.transpose(lines_from(all_s, base + channels, share))
    taps_out[...] = table[:KERNEL]
    conv_bias_out[...] = table[KERNEL]
    gain_out[...] = table[KERNEL + 1]
    bias_out[...] = table[KERNEL + 2]
    wide = sources * share
    up_bias_out[:wide] = table[KERNEL + 3]
    up_bias_out[wide:] = table[KERNEL + 4]
    base = base + channels + share
    lines = all_s[0, base : base + 16].astype(F32)
    for source in range(1, sources):
        lines = lines + all_s[source, base : base + 16].astype(F32)
    outs = (attn_gain_out, attn_bias_out, mlp_gain_out, mlp_bias_out, content_out, position_out, down_bias_out, merge_bias_out)
    for line, out in enumerate(outs):
        out[...] = lines[line]
    base = base + 16
    merge_share = 2 * D // (4 * sources)
    head_share = D // (4 * sources)
    for source in range(sources):
        for tile in range(4):
            lanes = slice(tile * LANES, (tile + 1) * LANES)
            at = base + tile * merge_share
            merge_out[source * merge_share : (source + 1) * merge_share, lanes] = all_s[
                source, at : at + merge_share
            ].astype(F32)
            at = base + 4 * merge_share + tile * head_share
            outw_out[source * head_share : (source + 1) * head_share, lanes] = all_s[
                source, at : at + head_share
            ].astype(F32)


def moved(block, axis, bits):
    count = lax.axis_size(axis)
    return lax.ppermute(block, axis, [(index, index ^ bits) for index in range(count)])


def over_streams(packs):
    return [packs[0]] + [moved(packs[bits], "stream", bits) for bits in range(1, lax.axis_size("stream"))]


def near_blocks(block):
    return [block] + [moved(block, "tm", bits) for bits in range(2, lax.axis_size("tm"), 2)]


def far_blocks(near):
    far = [moved(part, "tm", 1) for part in near]
    return [part for pair in zip(near, far) for part in pair]


def far_stack(near):
    stack = jnp.stack(near)
    return stack, moved(stack, "tm", 1)


def head_device(
    frames,
    lengths,
    cotangent,
    ln_attn_gain,
    ln_attn_bias,
    ln_mlp_gain,
    ln_mlp_bias,
    qkv_weight,
    content_bias,
    position_bias,
    pos_weight,
    out_weight,
    up_weight,
    up_bias,
    gate_norm_gain,
    gate_norm_bias,
    conv_kernel,
    conv_bias,
    down_weight,
    down_bias,
    merge_weight,
    merge_bias,
):
    count = lax.axis_size("tm")
    quarters = lax.axis_size("stream")
    own = frames.shape[1]
    total = own * count
    folded = total + total // 2
    padded = folded + 4 * MARGIN
    share = HALF // (quarters * count)
    channels = HALF // count
    quarter = D // quarters
    own_frames = frames[0]
    own_cotangent = cotangent[0]

    whole, late = Part(), Part(late=True)
    near = near_blocks(jnp.concatenate([own_frames, own_cotangent], axis=1))
    up_own, table, qkv_own, pos_own, bias_own = kernel_call(
        select_kernel,
        [
            ((D, 3 * LANES), BF16),
            ((2, 8 + KERNEL + 1, LANES), F32),
            ((D, 3 * LANES), BF16),
            ((D, LANES), BF16),
            ((8, LANES), F32),
        ],
        10 * "v",
    )(
        up_weight,
        up_bias,
        gate_norm_gain,
        gate_norm_bias,
        conv_bias,
        conv_kernel,
        qkv_weight,
        pos_weight,
        content_bias,
        position_bias,
    )
    near, up_own = lax.optimization_barrier((near, up_own))
    blocks = far_blocks(near)
    frequency = jnp.exp(jnp.arange(D // 2, dtype=F32) * (-2.0 * math.log(10000.0) / D))
    coarse = jnp.arange(0, total, BLOCK, dtype=F32)[:, None] * frequency[None]
    fine = jnp.arange(BLOCK, dtype=F32)[:, None] * frequency[None]
    coarse_table = jnp.concatenate([jnp.sin(coarse), jnp.cos(coarse)], axis=1)
    fine_table = jnp.concatenate([jnp.sin(fine), jnp.cos(fine)], axis=1)

    n_attn, n_mlp, hat, q_position, query, key, value, prob, attn, stats = kernel_call(
        attend_kernel,
        [
            ((total, D), BF16, 1),
            ((total, D), BF16, 1),
            ((total, D), BF16, 1),
            ((total, LANES), BF16, 1),
            ((total, LANES + D), BF16, 1),
            ((total, LANES + D), BF16, 1),
            ((total, LANES), BF16, 1),
            ((total, total), BF16, 1),
            ((total, LANES), F32, 1),
            ((total, LANES), F32, 1),
        ],
        [
            "s",
            blocks_part(0),
            *"vvvvvvvvv",
            Part((D, HALF), lambda refs, buffer: [(refs[0].at[:, pl.ds(HALF, HALF)], buffer)], late=True),
            "v",
        ],
        bounds=True,
    )(
        lengths,
        *blocks,
        ln_attn_gain,
        ln_attn_bias,
        ln_mlp_gain,
        ln_mlp_bias,
        qkv_own,
        pos_own,
        bias_own,
        coarse_table,
        fine_table,
        up_weight,
        up_bias,
    )

    def own_down(refs, buffer):
        place = lax.axis_index("tm")
        stride = HALF // quarters
        return [
            (
                refs[0].at[pl.ds(pl.multiple_of(part * stride + share * place, 16), share)],
                buffer.at[pl.ds(part * share, share)],
            )
            for part in range(quarters)
        ]

    mixed, gate_pre, grad_y, slope, gate_hat, early_pack, vectors, first_lines = kernel_call(
        mlp_first_kernel,
        [
            ((count, own + 16, 2 * LANES), BF16, 1),
            ((folded, LANES), BF16, 1),
            ((folded, LANES), BF16, 1),
            ((folded, LANES), BF16, 1),
            ((folded, LANES), BF16, 1),
            ((quarters, 8 * share, LANES), BF16, 1),
            ((channels, LANES), F32),
            ((8, D), F32),
        ],
        [
            "s",
            whole,
            "v",
            "v",
            whole,
            blocks_part(1, late=True),
            rows_part(D, D, late=True),
            Part((2 * LANES, D), own_down, late=True),
            Part(late=True),
        ],
        [
            ((folded, LANES), F32),
            ((folded, LANES), F32),
            ((total, 2 * LANES), BF16),
            ((folded, LANES), F32),
            ((folded, LANES), F32),
            ((padded, LANES), F32),
            ((padded, LANES), F32),
            ((folded, LANES), F32),
            ((folded, LANES), F32),
            ((total, D), BF16),
            ((total, 2 * LANES), BF16),
            ((2, 32, 8, LANES), F32),
            ((2, 32, 8, LANES), F32),
            ((2, 32, 8, LANES), F32),
            ((total, LANES), F32),
            ((3, WINDOW + 2 * MARGIN, LANES), F32),
            ((3, WINDOW + 2 * MARGIN, LANES), F32),
        ],
        bounds=True,
    )(lengths, n_mlp, up_own, table, stats, *blocks, merge_weight, down_weight, attn)
    mixed_own = lax.all_to_all(mixed, "tm", 0, 0, tiled=True)

    def own_head(refs, buffer):
        at = pl.ds(pl.multiple_of(lax.axis_index("tm") * HEAD, HEAD), HEAD)
        return [(refs[0].at[at], buffer.at[pl.ds(0, HEAD)])]

    branch, from_attn, *head_packs, head_lines = kernel_call(
        attend_back_kernel,
        [
            ((total, D), BF16, 1),
            ((total, D), BF16, 1),
            *([((4 * HEAD + 8 * share, LANES), BF16, 1)] * quarters),
            ((8, D), F32),
        ],
        [
            blocks_part(1),
            rows_part(0, D),
            Part((LANES, D), own_head),
            whole,
            late,
            late,
            late,
            "v",
            "v",
            late,
            Part((total, LANES), lambda refs, buffer: [(refs[0].at[:, pl.ds(0, LANES)], buffer)], late=True),
            late,
            late,
            late,
            late,
            "v",
            late,
        ],
        [
            ((total, LANES), BF16),
            ((total, total), BF16),
            ((total, D), BF16),
            ((total, 3 * LANES), BF16),
            ((4 * HEAD, D), F32),
        ],
    )(
        *blocks,
        merge_weight,
        out_weight,
        attn,
        value,
        prob,
        key,
        coarse_table,
        fine_table,
        pos_own,
        query,
        n_attn,
        q_position,
        qkv_own,
        hat,
        ln_attn_gain,
        early_pack,
    )
    head_parts = over_streams(head_packs)
    mixed_own, _ = lax.optimization_barrier((mixed_own, head_lines))
    out_rows, joined = kernel_call(
        output_kernel,
        [((own, D), BF16), ((count, 256, own), BF16)],
        "vvvvvvv",
        megas=24,
    )(own_frames, mixed_own, out_weight, down_weight, down_bias, merge_weight, merge_bias)
    joined_all = lax.all_to_all(joined, "tm", 0, 0, tiled=True)
    gate_pre, _ = lax.optimization_barrier((gate_pre, joined))
    late_rows = 5 * share + 16 + 3 * D // count
    pre, same, apart, own_lines, up_columns = kernel_call(
        mlp_second_kernel,
        [
            ((total, 3 * LANES), BF16, 1),
            ((count // 2, own, D), BF16, 1),
            ((count // 2, own, D), BF16, 1),
            ((8, D), F32),
            ((channels, LANES), F32),
        ],
        [
            Part(
                (count, 2 * total // BLOCK, 2 * LANES),
                lambda refs, buffer: [(refs[0].at[:, pl.ds(own, 2 * total // BLOCK)], buffer)],
            ),
            *([whole] * 4),
            late,
            late,
            "v",
            late,
        ],
        [((total, LANES), F32)],
    )(mixed_own, gate_pre, grad_y, slope, gate_hat, up_own, hat, ln_mlp_gain, from_attn)
    sibling = moved(apart, "tm", 1)
    pre, joined_all = lax.optimization_barrier((pre, joined_all))
    (late_pack,) = kernel_call(
        late_pack_kernel,
        [((quarters, late_rows, LANES), BF16, 1)],
        [
            Part(
                (total, 2 * LANES),
                lambda refs, buffer: [(refs[0].at[:, pl.ds(LANES, 2 * LANES)], buffer)],
            ),
            whole,
            whole,
            whole,
            blocks_part(1),
            *"vvvvv",
        ],
    )(pre, n_mlp, joined_all, branch, *blocks, vectors, up_columns, first_lines, head_lines, own_lines)
    late_pack, head_parts = lax.optimization_barrier((late_pack, head_parts))
    late_moved = lax.all_to_all(late_pack, "stream", 0, 0, tiled=True)
    (early_part,) = kernel_call(add_kernel, [((4 * HEAD + 8 * share, LANES), BF16)], quarters * "v", megas=24)(
        *head_parts
    )
    early_near = near_blocks(early_part)
    pairs = kernel_call(pair_kernel, [((own, D), BF16)] * (count // 2), "vv", megas=24)(same, sibling)
    sums = [pairs[0]] + [moved(pairs[slot], "tm", 2 * slot) for slot in range(1, count // 2)]
    late_moved, early_near, sums = lax.optimization_barrier((late_moved, early_near, sums))
    (late_part,) = kernel_call(add_streams_kernel, [((late_rows, LANES), BF16)], "v", megas=24)(late_moved)
    late_near = near_blocks(late_part)
    early_all = far_stack(early_near)
    (grad_frames,) = kernel_call(frames_kernel, [((own, D), F32)], (2 + count // 2) * "v", megas=24)(
        own_frames, own_cotangent, *sums
    )
    grad_qkv, grad_pos, grad_down, half_up = kernel_call(
        early_kernel,
        [
            ((quarter, 3 * D), F32),
            ((quarter, D), F32),
            ((HALF // quarters, D), F32),
            ((quarter, 2 * HALF), F32, 1, (quarter, HALF), lambda ref: ref.at[:, pl.ds(0, HALF)]),
        ],
        "vv",
        [((count, 4 * HEAD + 8 * share, LANES), BF16)],
        megas=24,
    )(*early_all)
    late_near, grad_frames, grad_pos = lax.optimization_barrier((late_near, grad_frames, grad_pos))
    late_parts = far_stack(late_near)
    late = kernel_call(
        late_kernel,
        [((quarter,), F32)] * 6
        + [
            ((quarter, D), F32),
            ((quarter, 2 * HALF), F32, 1, (quarter, HALF), lambda ref: ref.at[:, pl.ds(HALF, HALF)]),
            ((2 * HALF // quarters,), F32),
            ((HALF // quarters,), F32),
            ((HALF // quarters,), F32),
            ((KERNEL, HALF // quarters), F32),
            ((HALF // quarters,), F32),
            ((quarter,), F32),
            ((2 * D // quarters, D), F32),
            ((quarter,), F32),
        ],
        "kvv",
        [((count,) + late_part.shape, BF16)],
        megas=24,
        aliases={0: 7},
    )(half_up, *late_parts)
    return (
        out_rows[None],
        grad_frames[None],
        *late[:4],
        grad_qkv,
        *late[4:6],
        grad_pos,
        *late[6:13],
        grad_down,
        *late[13:],
    )


def per_device(*operands):
    fits = (
        lax.axis_size("tm") == HEADS
        and lax.axis_size("stream") * LANES == D
        and operands[0].shape[1] == BLOCK
    )
    return head_device(*operands) if fits else frame_device(*operands)


def solution(mesh):
    return jax.shard_map(
        per_device,
        mesh=mesh,
        in_specs=(
            P("stream", "tm", None),
            P("stream", None),
            P("stream", "tm", None),
            P(),
            P(),
            P(),
            P(),
            P(),
            P(),
            P(),
            P(),
            P(),
            P(),
            P(),
            P(),
            P(),
            P(),
            P(),
            P(),
            P(),
            P(),
            P(),
        ),
        out_specs=(
            P("stream", "tm", None),
            P("stream", "tm", None),
            P("stream"),
            P("stream"),
            P("stream"),
            P("stream"),
            P("stream", None),
            P("stream"),
            P("stream"),
            P("stream", None),
            P("stream", None),
            P("stream", None),
            P("stream"),
            P("stream"),
            P("stream"),
            P(None, "stream"),
            P("stream"),
            P("stream", None),
            P("stream"),
            P("stream", None),
            P("stream"),
        ),
        check_vma=False,
    )
```

```python
import math

import jax
import jax.numpy as jnp
from jax import lax
from jax.experimental import pallas as pl
from jax.experimental.pallas import tpu as pltpu
from jax.sharding import PartitionSpec as P

D = 512
HEADS = 8
HEAD = 64
KERNEL = 31
ITEMS = 5
HALF = 1536


EPS = 1e-05
MASKED = -1e30


def extended(block, sides, width):
    for axis, dim in sides:
        count = lax.axis_size(axis)
        forward = [(i, i + 1) for i in range(count - 1)]
        backward = [(target, source) for source, target in forward]
        low = lax.ppermute(
            lax.slice_in_dim(block, block.shape[dim] - width, None, axis=dim), axis, forward
        )
        high = lax.ppermute(lax.slice_in_dim(block, 0, width, axis=dim), axis, backward)
        block = jnp.concatenate([low, block, high], axis=dim)
    return block


def norm_rows(inputs, scale_row, shift_row):
    row_mean = jnp.mean(inputs, axis=-1, keepdims=True)
    centred = inputs - row_mean
    spread = jnp.mean(centred * centred, axis=-1, keepdims=True)
    return centred * lax.rsqrt(spread + EPS) * scale_row + shift_row


def gelu_exact(inputs):
    return jax.nn.gelu(inputs, approximate=False)


def frame_info(lengths, offset, extent):
    item_ends = jnp.cumsum(lengths)
    first_table = jnp.concatenate([item_ends - lengths, item_ends[-1:]])
    frame_index = offset + jnp.arange(extent, dtype=jnp.int32)
    item_of = jnp.sum((frame_index[:, None] >= item_ends[None, :]).astype(jnp.int32), axis=1)
    labels = jnp.arange(ITEMS + 1, dtype=jnp.int32)
    first_frame = jnp.sum(
        jnp.where(item_of[:, None] == labels[None, :], first_table[None, :], 0), axis=1
    )
    return (frame_index, item_of, frame_index - first_frame)


def angles(place_in):
    frequency = jnp.exp(jnp.arange(D // 2, dtype=jnp.float32) * (-2.0 * math.log(10000.0) / D))
    phase_angle = place_in.astype(jnp.float32)[:, None] * frequency[None, :]
    return (jnp.sin(phase_angle), jnp.cos(phase_angle))


def rel_query(projected, sine_rows, cosine_rows):
    half_size = projected.shape[-1] // 2
    first_half = projected[..., :half_size]
    second_half = projected[..., half_size:]
    sine_wide = sine_rows[:, None, :]
    cosine_wide = cosine_rows[:, None, :]
    return jnp.concatenate(
        [
            first_half * sine_wide + second_half * cosine_wide,
            second_half * sine_wide - first_half * cosine_wide,
        ],
        axis=-1,
    )


def step_size(extent):
    return math.gcd(extent, 512)


def score_block(q_content, q_rel, query_item, query_frame, key_block, key_start, lengths):
    extent = key_block.shape[0]
    key_frame, key_item, key_place = frame_info(lengths, key_start, extent)
    sine_rows, cosine_rows = angles(key_place)
    k_rel = jnp.concatenate([cosine_rows, sine_rows], axis=1).astype(jnp.bfloat16)
    raw_scores = jnp.einsum(
        "qhe,khe->hqk",
        q_content,
        key_block.reshape(extent, HEADS, HEAD),
        preferred_element_type=jnp.float32,
    )
    raw_scores = raw_scores + jnp.einsum(
        "qhc,kc->hqk", q_rel, k_rel, preferred_element_type=jnp.float32
    )
    allowed = (query_item[:, None] == key_item[None, :]) & (
        (query_item[:, None] < ITEMS) | (query_frame[:, None] == key_frame[None, :])
    )
    return (raw_scores, allowed, k_rel)


def block_grads(
    q_content,
    q_rel,
    query_item,
    query_frame,
    grad_out,
    log_total,
    delta_rows,
    key_block,
    value_block,
    key_start,
    lengths,
):
    extent = key_block.shape[0]
    raw_scores, allowed, k_rel = score_block(
        q_content, q_rel, query_item, query_frame, key_block, key_start, lengths
    )
    prob_rows = jnp.where(allowed[None], jnp.exp(raw_scores * 0.125 - log_total[:, :, None]), 0.0)
    grad_prob = jnp.einsum(
        "qhe,khe->hqk",
        grad_out,
        value_block.reshape(extent, HEADS, HEAD),
        preferred_element_type=jnp.float32,
    )
    grad_raw = (prob_rows * (grad_prob - delta_rows[:, :, None]) * 0.125).astype(jnp.bfloat16)
    return (prob_rows.astype(jnp.bfloat16), grad_raw, k_rel)


def frame_device(
    frames,
    lengths,
    cotangent,
    ln_attn_gain,
    ln_attn_bias,
    ln_mlp_gain,
    ln_mlp_bias,
    qkv_weight,
    content_bias,
    position_bias,
    pos_weight,
    out_weight,
    up_weight,
    up_bias,
    gate_norm_gain,
    gate_norm_bias,
    conv_kernel,
    conv_bias,
    down_weight,
    down_bias,
    merge_weight,
    merge_bias,
):
    row_count = frames.shape[1]
    cycle_size = lax.axis_size("tm")
    offset = lax.axis_index("tm") * row_count
    stream_lengths = lengths[0]
    inputs = frames[0].astype(jnp.float32)
    frame_index, item_of, place_in = frame_info(stream_lengths, offset, row_count)
    sine_rows, cosine_rows = angles(place_in)
    attn_norm, attn_pull = jax.vjp(
        norm_rows, inputs, ln_attn_gain.astype(jnp.float32), ln_attn_bias.astype(jnp.float32)
    )
    mlp_norm, mlp_pull = jax.vjp(
        norm_rows, inputs, ln_mlp_gain.astype(jnp.float32), ln_mlp_bias.astype(jnp.float32)
    )
    attn_norm_low = attn_norm.astype(jnp.bfloat16)
    mlp_norm_low = mlp_norm.astype(jnp.bfloat16)
    qkv_rows = jnp.dot(attn_norm_low, qkv_weight, preferred_element_type=jnp.float32)
    query_rows = qkv_rows[:, :D]
    key_rows = qkv_rows[:, D : 2 * D].astype(jnp.bfloat16)
    value_rows = qkv_rows[:, 2 * D :].astype(jnp.bfloat16)
    q_content = (query_rows + content_bias.astype(jnp.float32)).astype(jnp.bfloat16)
    q_position = (query_rows + position_bias.astype(jnp.float32)).astype(jnp.bfloat16)
    content_heads = q_content.reshape(row_count, HEADS, HEAD)
    position_heads = q_position.reshape(row_count, HEADS, HEAD)
    pos_heads = pos_weight.reshape(D, HEADS, HEAD)
    projected = jnp.einsum(
        "the,che->thc", position_heads, pos_heads, preferred_element_type=jnp.float32
    )
    q_rel = rel_query(projected, sine_rows, cosine_rows).astype(jnp.bfloat16)
    start_state = (
        jnp.full((HEADS, row_count), MASKED, jnp.float32),
        jnp.zeros((HEADS, row_count), jnp.float32),
        jnp.zeros((HEADS, row_count, HEAD), jnp.float32),
    )
    fold_state = start_state
    key_piece = lax.all_gather(key_rows, "tm", axis=0, tiled=True)
    value_piece = lax.all_gather(value_rows, "tm", axis=0, tiled=True)
    extent = key_piece.shape[0]
    step_rows = step_size(extent)

    def forward_one_step(inner_state, step_index):
        row_top, row_total, row_acc = inner_state
        key_block = lax.dynamic_slice_in_dim(key_piece, step_index * step_rows, step_rows, 0)
        value_block = lax.dynamic_slice_in_dim(value_piece, step_index * step_rows, step_rows, 0)
        raw_scores, allowed, k_rel = score_block(
            content_heads,
            q_rel,
            item_of,
            frame_index,
            key_block,
            step_index * step_rows,
            stream_lengths,
        )
        scaled = jnp.where(allowed[None], raw_scores * 0.125, MASKED)
        new_top = jnp.maximum(row_top, jnp.max(scaled, axis=2))
        weight = jnp.where(allowed[None], jnp.exp(scaled - new_top[:, :, None]), 0.0)
        factor = jnp.exp(row_top - new_top)
        row_total = row_total * factor + jnp.sum(weight, axis=2)
        row_acc = row_acc * factor[:, :, None] + jnp.einsum(
            "hqk,khe->hqe",
            weight.astype(jnp.bfloat16),
            value_block.reshape(step_rows, HEADS, HEAD),
            preferred_element_type=jnp.float32,
        )
        return ((new_top, row_total, row_acc), None)

    fold_state, unused = lax.scan(
        forward_one_step, fold_state, jnp.arange(extent // step_rows, dtype=jnp.int32)
    )
    row_top, row_total, row_acc = fold_state
    attn_heads = row_acc / row_total[:, :, None]
    log_total = row_top + jnp.log(row_total)
    attn_low = jnp.transpose(attn_heads, (1, 0, 2)).reshape(row_count, D).astype(jnp.bfloat16)
    branch_attn = jnp.dot(attn_low, out_weight, preferred_element_type=jnp.float32).astype(
        jnp.bfloat16
    )
    hidden_pre = jnp.dot(
        mlp_norm_low, up_weight, preferred_element_type=jnp.float32
    ) + up_bias.astype(jnp.float32)
    hidden, gelu_pull = jax.vjp(gelu_exact, hidden_pre)
    gate_half = hidden[:, :HALF]
    conv_norm, conv_pull = jax.vjp(
        norm_rows,
        hidden[:, HALF:],
        gate_norm_gain.astype(jnp.float32),
        gate_norm_bias.astype(jnp.float32),
    )
    conv_in = conv_norm.astype(jnp.bfloat16)
    half_width = KERNEL // 2
    conv_wide = extended(conv_in, (("tm", 0),), half_width)
    wide_frame, wide_item, wide_place = frame_info(
        stream_lengths, offset - half_width, row_count + 2 * half_width
    )
    kernel_rows = conv_kernel.astype(jnp.float32)
    conv_out = conv_bias.astype(jnp.float32) + jnp.zeros_like(gate_half)
    for tap_index in range(KERNEL):
        same_item = (wide_item[tap_index : tap_index + row_count] == item_of)[:, None]
        conv_out = (
            conv_out
            + jnp.where(
                same_item, conv_wide[tap_index : tap_index + row_count].astype(jnp.float32), 0.0
            )
            * kernel_rows[tap_index]
        )
    gated_low = (gate_half * conv_out).astype(jnp.bfloat16)
    branch_mlp = (
        jnp.dot(gated_low, down_weight, preferred_element_type=jnp.float32)
        + down_bias.astype(jnp.float32)
    ).astype(jnp.bfloat16)
    joined = jnp.concatenate([branch_attn, branch_mlp], axis=1)
    result = (
        inputs
        + jnp.dot(joined, merge_weight, preferred_element_type=jnp.float32)
        + merge_bias.astype(jnp.float32)
    )
    out_rows = result.astype(jnp.bfloat16)[None]
    grad_low = cotangent[0]
    grad_rows = grad_low.astype(jnp.float32)
    grad_merge_bias = jnp.sum(grad_rows, axis=0)
    grad_merge_weight = jnp.einsum(
        "tc,td->cd", joined, grad_low, preferred_element_type=jnp.float32
    )
    grad_joined = jnp.einsum(
        "td,cd->tc", grad_low, merge_weight, preferred_element_type=jnp.float32
    )
    grad_attn_branch = grad_joined[:, :D].astype(jnp.bfloat16)
    grad_mlp_branch = grad_joined[:, D:].astype(jnp.bfloat16)
    grad_down_weight = jnp.einsum(
        "tc,td->cd", gated_low, grad_mlp_branch, preferred_element_type=jnp.float32
    )
    grad_down_bias = jnp.sum(grad_mlp_branch.astype(jnp.float32), axis=0)
    grad_gated = jnp.einsum(
        "td,cd->tc", grad_mlp_branch, down_weight, preferred_element_type=jnp.float32
    )
    grad_gate_half = grad_gated * conv_out
    grad_conv_out = (grad_gated * gate_half).astype(jnp.bfloat16)
    grad_conv_rows = grad_conv_out.astype(jnp.float32)
    grad_conv_bias = jnp.sum(grad_conv_rows, axis=0)
    grad_wide = extended(grad_conv_out, (("tm", 0),), half_width)
    kernel_list = []
    grad_conv_in = jnp.zeros_like(grad_conv_rows)
    for tap_index in range(KERNEL):
        same_item = (wide_item[tap_index : tap_index + row_count] == item_of)[:, None]
        kernel_list.append(
            jnp.sum(
                jnp.where(
                    same_item, conv_wide[tap_index : tap_index + row_count].astype(jnp.float32), 0.0
                )
                * grad_conv_rows,
                axis=0,
            )
        )
        back_start = 2 * half_width - tap_index
        back_item = (wide_item[back_start : back_start + row_count] == item_of)[:, None]
        grad_conv_in = (
            grad_conv_in
            + jnp.where(
                back_item, grad_wide[back_start : back_start + row_count].astype(jnp.float32), 0.0
            )
            * kernel_rows[tap_index]
        )
    grad_conv_kernel = jnp.stack(kernel_list)
    grad_second, grad_gate_norm_gain, grad_gate_norm_bias = conv_pull(grad_conv_in)
    (grad_pre_rows,) = gelu_pull(jnp.concatenate([grad_gate_half, grad_second], axis=1))
    grad_pre = grad_pre_rows.astype(jnp.bfloat16)
    grad_up_bias = jnp.sum(grad_pre.astype(jnp.float32), axis=0)
    grad_up_weight = jnp.einsum(
        "tc,tf->cf", mlp_norm_low, grad_pre, preferred_element_type=jnp.float32
    )
    grad_mlp_norm = jnp.einsum("tf,cf->tc", grad_pre, up_weight, preferred_element_type=jnp.float32)
    grad_out_weight = jnp.einsum(
        "tc,td->cd", attn_low, grad_attn_branch, preferred_element_type=jnp.float32
    )
    grad_attn_low = jnp.einsum(
        "td,cd->tc", grad_attn_branch, out_weight, preferred_element_type=jnp.float32
    ).astype(jnp.bfloat16)
    grad_out_heads = grad_attn_low.reshape(row_count, HEADS, HEAD)
    delta_rows = jnp.sum(
        jnp.transpose(grad_out_heads.astype(jnp.float32), (1, 0, 2)) * attn_heads, axis=2
    )
    total_frames = row_count * cycle_size
    back_start_state = (
        jnp.zeros((row_count, HEADS, HEAD), jnp.float32),
        jnp.zeros((row_count, HEADS, D), jnp.float32),
        jnp.zeros((total_frames, D), jnp.float32),
        jnp.zeros((total_frames, D), jnp.float32),
    )
    back_key_piece = lax.all_gather(key_rows, "tm", axis=0, tiled=True)
    back_value_piece = lax.all_gather(value_rows, "tm", axis=0, tiled=True)
    extent = back_key_piece.shape[0]
    back_step_rows = step_size(extent)

    def back_one_step(inner_state, step_index):
        grad_content, grad_rel = inner_state
        key_block = lax.dynamic_slice_in_dim(
            back_key_piece, step_index * back_step_rows, back_step_rows, 0
        )
        value_block = lax.dynamic_slice_in_dim(
            back_value_piece, step_index * back_step_rows, back_step_rows, 0
        )
        prob_low, grad_raw, k_rel = block_grads(
            content_heads,
            q_rel,
            item_of,
            frame_index,
            grad_out_heads,
            log_total,
            delta_rows,
            key_block,
            value_block,
            step_index * back_step_rows,
            stream_lengths,
        )
        grad_content = grad_content + jnp.einsum(
            "hqk,khe->qhe",
            grad_raw,
            key_block.reshape(back_step_rows, HEADS, HEAD),
            preferred_element_type=jnp.float32,
        )
        grad_rel = grad_rel + jnp.einsum(
            "hqk,kc->qhc", grad_raw, k_rel, preferred_element_type=jnp.float32
        )
        key_part = jnp.einsum(
            "hqk,qhe->khe", grad_raw, content_heads, preferred_element_type=jnp.float32
        ).reshape(back_step_rows, D)
        value_part = jnp.einsum(
            "hqk,qhe->khe", prob_low, grad_out_heads, preferred_element_type=jnp.float32
        ).reshape(back_step_rows, D)
        return ((grad_content, grad_rel), (key_part, value_part))

    inner_state, block_parts = lax.scan(
        back_one_step,
        (back_start_state[0], back_start_state[1]),
        jnp.arange(extent // back_step_rows, dtype=jnp.int32),
    )
    key_all = block_parts[0].reshape(extent, D)
    value_all = block_parts[1].reshape(extent, D)
    grad_content, grad_rel, key_all, value_all = (
        inner_state[0],
        inner_state[1],
        key_all,
        value_all,
    )
    grad_keys, grad_values = (
        lax.psum_scatter(key_all, "tm", scatter_dimension=0, tiled=True),
        lax.psum_scatter(value_all, "tm", scatter_dimension=0, tiled=True),
    )
    half_size = D // 2
    rel_first = grad_rel[..., :half_size]
    rel_second = grad_rel[..., half_size:]
    sine_wide = sine_rows[:, None, :]
    cosine_wide = cosine_rows[:, None, :]
    grad_projected = jnp.concatenate(
        [
            rel_first * sine_wide - rel_second * cosine_wide,
            rel_first * cosine_wide + rel_second * sine_wide,
        ],
        axis=-1,
    ).astype(jnp.bfloat16)
    grad_pos_weight = jnp.einsum(
        "thc,the->che", grad_projected, position_heads, preferred_element_type=jnp.float32
    ).reshape(D, D)
    grad_q_position = jnp.einsum(
        "thc,che->the", grad_projected, pos_heads, preferred_element_type=jnp.float32
    )
    grad_content_bias = jnp.sum(grad_content, axis=0).reshape(D)
    grad_position_bias = jnp.sum(grad_q_position, axis=0).reshape(D)
    grad_query = (grad_content + grad_q_position).reshape(row_count, D).astype(jnp.bfloat16)
    grad_qkv = jnp.concatenate(
        [grad_query, grad_keys.astype(jnp.bfloat16), grad_values.astype(jnp.bfloat16)], axis=1
    )
    grad_qkv_weight = jnp.einsum(
        "tc,tf->cf", attn_norm_low, grad_qkv, preferred_element_type=jnp.float32
    )
    grad_attn_norm = jnp.einsum(
        "tf,cf->tc", grad_qkv, qkv_weight, preferred_element_type=jnp.float32
    )
    grad_from_attn, grad_ln_attn_gain, grad_ln_attn_bias = attn_pull(grad_attn_norm)
    grad_from_mlp, grad_ln_mlp_gain, grad_ln_mlp_bias = mlp_pull(grad_mlp_norm)
    grad_inputs = grad_rows + grad_from_attn + grad_from_mlp
    weight_grads = (
        grad_ln_attn_gain,
        grad_ln_attn_bias,
        grad_ln_mlp_gain,
        grad_ln_mlp_bias,
        grad_qkv_weight,
        grad_content_bias,
        grad_position_bias,
        grad_pos_weight,
        grad_out_weight,
        grad_up_weight,
        grad_up_bias,
        grad_gate_norm_gain,
        grad_gate_norm_bias,
        grad_conv_kernel,
        grad_conv_bias,
        grad_down_weight,
        grad_down_bias,
        grad_merge_weight,
        grad_merge_bias,
    )
    summed = lax.psum(
        (
            weight_grads[0],
            weight_grads[1],
            weight_grads[2],
            weight_grads[3],
            weight_grads[4],
            weight_grads[5],
            weight_grads[6],
            weight_grads[7],
            weight_grads[8],
            weight_grads[9],
            weight_grads[10],
            weight_grads[11],
            weight_grads[12],
            weight_grads[13],
            weight_grads[14],
            weight_grads[15],
            weight_grads[16],
            weight_grads[17],
            weight_grads[18],
        ),
        "tm",
    )
    shares = (
        lax.psum_scatter(
            summed[0].astype(jnp.bfloat16), "stream", scatter_dimension=0, tiled=True
        ).astype(jnp.float32),
        lax.psum_scatter(
            summed[1].astype(jnp.bfloat16), "stream", scatter_dimension=0, tiled=True
        ).astype(jnp.float32),
        lax.psum_scatter(
            summed[2].astype(jnp.bfloat16), "stream", scatter_dimension=0, tiled=True
        ).astype(jnp.float32),
        lax.psum_scatter(
            summed[3].astype(jnp.bfloat16), "stream", scatter_dimension=0, tiled=True
        ).astype(jnp.float32),
        lax.psum_scatter(
            summed[4].astype(jnp.bfloat16), "stream", scatter_dimension=0, tiled=True
        ).astype(jnp.float32),
        lax.psum_scatter(
            summed[5].astype(jnp.bfloat16), "stream", scatter_dimension=0, tiled=True
        ).astype(jnp.float32),
        lax.psum_scatter(
            summed[6].astype(jnp.bfloat16), "stream", scatter_dimension=0, tiled=True
        ).astype(jnp.float32),
        lax.psum_scatter(
            summed[7].astype(jnp.bfloat16), "stream", scatter_dimension=0, tiled=True
        ).astype(jnp.float32),
        lax.psum_scatter(
            summed[8].astype(jnp.bfloat16), "stream", scatter_dimension=0, tiled=True
        ).astype(jnp.float32),
        lax.psum_scatter(
            summed[9].astype(jnp.bfloat16), "stream", scatter_dimension=0, tiled=True
        ).astype(jnp.float32),
        lax.psum_scatter(
            summed[10].astype(jnp.bfloat16), "stream", scatter_dimension=0, tiled=True
        ).astype(jnp.float32),
        lax.psum_scatter(
            summed[11].astype(jnp.bfloat16), "stream", scatter_dimension=0, tiled=True
        ).astype(jnp.float32),
        lax.psum_scatter(
            summed[12].astype(jnp.bfloat16), "stream", scatter_dimension=0, tiled=True
        ).astype(jnp.float32),
        lax.psum_scatter(
            summed[13].astype(jnp.bfloat16), "stream", scatter_dimension=1, tiled=True
        ).astype(jnp.float32),
        lax.psum_scatter(
            summed[14].astype(jnp.bfloat16), "stream", scatter_dimension=0, tiled=True
        ).astype(jnp.float32),
        lax.psum_scatter(
            summed[15].astype(jnp.bfloat16), "stream", scatter_dimension=0, tiled=True
        ).astype(jnp.float32),
        lax.psum_scatter(
            summed[16].astype(jnp.bfloat16), "stream", scatter_dimension=0, tiled=True
        ).astype(jnp.float32),
        lax.psum_scatter(
            summed[17].astype(jnp.bfloat16), "stream", scatter_dimension=0, tiled=True
        ).astype(jnp.float32),
        lax.psum_scatter(
            summed[18].astype(jnp.bfloat16), "stream", scatter_dimension=0, tiled=True
        ).astype(jnp.float32),
    )
    return (out_rows, grad_inputs[None]) + tuple(shares)


LANES = 128
LOW = LANES // 2
BLOCK = 128
TALL = 256
WINDOW = 64
MARGIN = 16
BOUNDS = 16
MEGA = 1024 * 1024
F32 = jnp.float32
BF16 = jnp.bfloat16


def dot_nn(left, right):
    return jnp.dot(left, right, preferred_element_type=F32)


def dot_nt(left, right):
    return lax.dot_general(left, right, (((1,), (1,)), ((), ())), preferred_element_type=F32)


def dot_tn(left, right):
    return lax.dot_general(left, right, (((0,), (0,)), ((), ())), preferred_element_type=F32)


def rows_of(index, size, base=0):
    return pl.ds(pl.multiple_of(index * size, size) + base, size)


def line_of(ref):
    return ref[...].astype(F32).reshape(1, ref.shape[0])


def fold_rows(values):
    return jnp.sum(values.reshape(values.shape[0] // 8, 8, values.shape[1]), axis=0)


def one_row(values):
    return jnp.sum(values, axis=0, keepdims=True)


def turn(values):
    return pltpu.roll(values, LOW, 1)


def low_lanes(rows):
    return lax.broadcasted_iota(jnp.int32, (rows, LANES), 1) < LOW


def centre_rows(inputs):
    mean = jnp.mean(inputs, axis=-1, keepdims=True)
    centred = inputs - mean
    spread = jnp.mean(centred * centred, axis=-1, keepdims=True)
    return centred * lax.rsqrt(spread + EPS)


def gelu_parts(values):
    phi = 0.5 + 0.5 * lax.erf(values * math.sqrt(0.5))
    bell = jnp.exp(values * values * -0.5)
    return values * phi, phi + values * bell * (1.0 / math.sqrt(2.0 * math.pi))


class Part:
    def __init__(self, shape=None, pairs=None, refs=1, late=False):
        self.shape, self.pairs, self.refs, self.late = shape, pairs, refs, late

    def buffer(self, operand):
        return self.shape or operand.shape

    def copies(self, refs, buffer):
        return self.pairs(refs, buffer) if self.pairs else [(refs[0], buffer)]


def blocks_part(half, late=False):
    def pairs(refs, buffer):
        place = lax.axis_index("tm")
        return [
            (
                ref.at[:, pl.ds(half * D, D)],
                buffer.at[rows_of(lax.bitwise_xor(jnp.int32(apart), place), BLOCK)],
            )
            for apart, ref in enumerate(refs)
        ]

    return Part((HEADS * BLOCK, D), pairs, HEADS, late)


def rows_part(first, size, late=False):
    return Part((size, D), lambda refs, buffer: [(refs[0].at[pl.ds(first, size)], buffer)], late=late)


class Fetch:
    def __init__(self, pairs, buffer, sems, first):
        self.buffer, self.begun = buffer, False
        self.pending = [
            pltpu.make_async_copy(source, target, sems.at[first + index])
            for index, (source, target) in enumerate(pairs)
        ]

    def begin(self):
        if not self.begun:
            for copy in self.pending:
                copy.start()
        self.begun = True

    def __call__(self):
        self.begin()
        for copy in self.pending:
            copy.wait()
        self.pending = []
        return self.buffer


def begin(*fetches):
    for fetch in fetches:
        fetch.begin()


class Send:
    def __init__(self, buffer, target, sems):
        self.buffer, self.target, self.sems, self.copies = buffer, target, sems, []

    def go(self, *index):
        source, target = (self.buffer.at[index], self.target.at[index]) if index else (self.buffer, self.target)
        copy = pltpu.make_async_copy(source, target, self.sems[len(self.copies)])
        copy.start()
        self.copies.append(copy)

    def finish(self):
        if not self.copies:
            self.go()


SPACES = {"v": pltpu.VMEM, "s": pltpu.SMEM, "k": pl.ANY}


def kernel_call(body, out_shapes, plan, scratch=(), megas=58, bounds=False, aliases=None):
    def call(*operands):
        in_specs, buffers, at = [], [], 0
        for item in plan:
            if item == "f":
                in_specs.append(pl.BlockSpec(memory_space=pl.ANY))
                buffers.append(pltpu.VMEM(operands[at].shape, operands[at].dtype))
                at += 1
            elif isinstance(item, Part):
                in_specs += [pl.BlockSpec(memory_space=pl.ANY)] * item.refs
                buffers.append(pltpu.VMEM(item.buffer(operands[at]), operands[at].dtype))
                at += item.refs
            else:
                in_specs.append(pl.BlockSpec(memory_space=SPACES[item]))
                at += 1
        sent = [out for out in out_shapes if len(out) > 2]
        buffers += [pltpu.VMEM(out[3] if len(out) > 3 else out[0], out[1]) for out in sent]
        sem_count = 96
        extra = [pltpu.SMEM((BOUNDS,), jnp.int32)] if bounds else []

        def outer(*refs):
            inputs, rest = refs[: len(in_specs)], refs[len(in_specs) :]
            outputs, rest = rest[: len(out_shapes)], rest[len(out_shapes) :]
            held, rest = list(rest[: len(buffers)]), rest[len(buffers) :]
            sems, rest = rest[0], rest[1:]
            given, at, used = [], 0, 0
            for item in plan:
                if item == "f":
                    given.append(Fetch([(inputs[at], held[0])], held.pop(0), sems, used))
                    given[-1].begin()
                    used += 1
                    at += 1
                elif isinstance(item, Part):
                    buffer = held.pop(0)
                    pairs = item.copies(inputs[at : at + item.refs], buffer)
                    given.append(Fetch(pairs, buffer, sems, used))
                    if not item.late:
                        given[-1].begin()
                    used += len(pairs)
                    at += item.refs
                else:
                    given.append(inputs[at])
                    at += 1
            results = []
            for out, ref in zip(out_shapes, outputs):
                if len(out) > 2:
                    target = out[4](ref) if len(out) > 3 else ref
                    results.append(Send(held.pop(0), target, [sems.at[used + index] for index in range(4)]))
                    used += 4
                else:
                    results.append(ref)
            assert used <= sem_count
            given = [item() if kind == "f" else item for kind, item in zip(plan, given)]
            body(*given, *results, *rest)
            for item in given:
                if isinstance(item, Fetch):
                    item()
            sends = [item for item in results if isinstance(item, Send)]
            for item in sends:
                item.finish()
            for item in sends:
                for copy in item.copies:
                    copy.wait()

        return pl.pallas_call(
            outer,
            out_shape=[jax.ShapeDtypeStruct(out[0], out[1]) for out in out_shapes],
            in_specs=in_specs,
            out_specs=[pl.BlockSpec(memory_space=pl.ANY if len(out) > 2 else pltpu.VMEM) for out in out_shapes],
            scratch_shapes=buffers
            + [pltpu.SemaphoreType.DMA((sem_count,))]
            + [pltpu.VMEM(shape, kind) for shape, kind in scratch]
            + extra,
            input_output_aliases=aliases or {},
            compiler_params=pltpu.CompilerParams(vmem_limit_bytes=megas * MEGA),
            cost_estimate=pl.CostEstimate(flops=0, bytes_accessed=0, transcendentals=0),
        )(*operands)

    return call


def fill_bounds(lengths_ref, bounds_s, total):
    bounds_s[0] = jnp.int32(0)
    end = jnp.int32(0)
    for item in range(ITEMS):
        end = end + lengths_ref[0, item]
        bounds_s[item + 1] = end
    for item in range(ITEMS + 1, BOUNDS):
        bounds_s[item] = jnp.int32(total)


def select_kernel(
    up_ref,
    up_bias_ref,
    gain_ref,
    bias_ref,
    conv_bias_ref,
    taps_ref,
    qkv_ref,
    pos_ref,
    content_ref,
    position_ref,
    up_out,
    table_out,
    qkv_out,
    pos_out,
    bias_out,
):
    place = lax.axis_index("tm")
    quarters = lax.axis_size("stream")
    share = HALF // (quarters * lax.axis_size("tm"))
    lane = lax.broadcasted_iota(jnp.int32, (1, 2 * LANES), 1)
    channel = jnp.where(lane < LANES + LOW, lane, lane - LOW)
    group = jnp.zeros_like(channel)
    for quarter in range(1, quarters):
        group = group + (channel >= quarter * share).astype(jnp.int32)
    source = group * (HALF // quarters) + share * place + channel - group * share
    chosen = (lax.broadcasted_iota(jnp.int32, (HALF, 2 * LANES), 0) == source).astype(F32).astype(BF16)
    gate = dot_nn(up_ref[:, :HALF], chosen)
    conv = dot_nn(up_ref[:, HALF:], chosen)
    up_out[:, :LANES] = gate[:, :LANES].astype(BF16)
    up_out[:, LANES : 2 * LANES] = jnp.where(low_lanes(D), gate[:, LANES:], conv[:, LANES:]).astype(BF16)
    up_out[:, 2 * LANES :] = conv[:, :LANES].astype(BF16)
    up_bias = line_of(up_bias_ref)
    lines = jnp.concatenate(
        [
            up_bias[:, :HALF],
            up_bias[:, HALF:],
            line_of(gain_ref),
            line_of(bias_ref),
            line_of(conv_bias_ref),
            jnp.zeros((3, HALF), F32),
        ],
        axis=0,
    )
    lines = dot_nn(lines.astype(BF16), chosen)
    taps = dot_nn(taps_ref[...], chosen)
    for part in range(2):
        lanes = slice(part * LANES, (part + 1) * LANES)
        table_out[part, :8] = lines[:, lanes]
        table_out[part, 8 : 8 + KERNEL] = taps[:, lanes]
        table_out[part, 8 + KERNEL :] = jnp.zeros((1, LANES), F32)

    odd = lax.rem(place, 2) == 1

    def head_lanes(ref, base):
        at = pl.ds(pl.multiple_of(lax.div(place, 2) * LANES + base, LANES), LANES)
        values = ref[:, at].astype(F32)
        values = jnp.where(odd, turn(values), values)
        return jnp.where(low_lanes(values.shape[0]), values, 0.0)

    for part in range(3):
        qkv_out[:, part * LANES : (part + 1) * LANES] = head_lanes(qkv_ref, part * D).astype(BF16)
    pos_out[...] = head_lanes(pos_ref, 0).astype(BF16)
    bias_out[...] = jnp.zeros((8, LANES), F32)
    for line, ref in enumerate((content_ref, position_ref)):
        values = line_of(ref)
        picked = values[:, :LANES]
        for tile in range(1, D // LANES):
            picked = jnp.where(
                lax.div(place, 2) == tile, values[:, tile * LANES : (tile + 1) * LANES], picked
            )
        picked = jnp.where(odd, turn(picked), picked)
        bias_out[line : line + 1] = jnp.where(low_lanes(1), picked, 0.0)


def angle_rows(coarse_ref, fine_ref, block, rows):
    half = D // 2
    base = coarse_ref[pl.ds(block, 1)]
    base_sine, base_cosine = base[:, :half], base[:, half:]
    sine, cosine = fine_ref[rows, :half], fine_ref[rows, half:]
    return base_sine * cosine + base_cosine * sine, base_cosine * cosine - base_sine * sine


def item_codes(bounds_s, index):
    code = jnp.zeros_like(index)
    for item in range(1, ITEMS + 1):
        code = code + (index >= bounds_s[item]).astype(jnp.int32)
    return jnp.where(code < ITEMS, code, ITEMS + index)


def attend_kernel(
    lengths_ref,
    x_ref,
    attn_gain_ref,
    attn_bias_ref,
    mlp_gain_ref,
    mlp_bias_ref,
    qkv_ref,
    pos_ref,
    bias_ref,
    coarse_ref,
    fine_ref,
    up_ref,
    up_bias_ref,
    n_attn_out,
    n_mlp_out,
    hat_out,
    q_position_out,
    query_out,
    key_out,
    value_out,
    prob_out,
    attn_out,
    mean_out,
    rate_out,
    bounds_s,
):
    frames = n_attn_out.buffer.shape[0]
    half = D // 2
    fill_bounds(lengths_ref, bounds_s, frames)
    attn_gain, attn_bias = line_of(attn_gain_ref), line_of(attn_bias_ref)
    mlp_gain, mlp_bias = line_of(mlp_gain_ref), line_of(mlp_bias_ref)
    content, position = bias_ref[0:1], bias_ref[1:2]
    x_ref = x_ref()
    begin(up_ref)

    @pl.loop(0, frames // TALL, unroll=4)
    def _(block):
        rows = rows_of(block, TALL)
        for part in range(TALL // 32):
            at = pl.ds(pl.multiple_of(block * TALL + part * 32, 32), 32)
            hat = centre_rows(x_ref[at].astype(F32))
            hat_out.buffer[at] = hat.astype(BF16)
            n_attn_out.buffer[at] = (hat * attn_gain + attn_bias).astype(BF16)
            n_mlp_out.buffer[at] = (hat * mlp_gain + mlp_bias).astype(BF16)
        parts = dot_nn(n_attn_out.buffer[rows], qkv_ref[...])
        query = parts[:, :LANES]
        query_out.buffer[rows, :LANES] = ((query + content).astype(BF16).astype(F32) * 0.125).astype(BF16)
        q_position = (query + position).astype(BF16)
        q_position_out.buffer[rows] = q_position
        key_out.buffer[rows, :LANES] = parts[:, LANES : 2 * LANES].astype(BF16)
        value_out.buffer[rows] = parts[:, 2 * LANES :].astype(BF16)
        projected = dot_nt(q_position, pos_ref[...])
        for part in range(TALL // 32):
            at = pl.ds(pl.multiple_of(block * TALL + part * 32, 32), 32)
            inner = part * 32 % BLOCK
            sine, cosine = angle_rows(
                coarse_ref, fine_ref, block * (TALL // BLOCK) + part * 32 // BLOCK, slice(inner, inner + 32)
            )
            first = projected[part * 32 : part * 32 + 32, :half]
            second = projected[part * 32 : part * 32 + 32, half:]
            query_out.buffer[at, LANES : LANES + half] = ((first * sine + second * cosine) * 0.125).astype(BF16)
            query_out.buffer[at, LANES + half :] = ((second * sine - first * cosine) * 0.125).astype(BF16)
            key_out.buffer[at, LANES : LANES + half] = cosine.astype(BF16)
            key_out.buffer[at, LANES + half :] = sine.astype(BF16)

    for out in (n_attn_out, n_mlp_out, hat_out, q_position_out, query_out, key_out, value_out):
        out.go()
    up_ref = up_ref()
    up_bias = line_of(up_bias_ref)[:, HALF:]
    @pl.loop(0, frames // TALL, unroll=2)
    def _(block):
        values = dot_nn(n_mlp_out.buffer[rows_of(block, TALL)], up_ref[...])
        for part in range(TALL // 16):
            pre = values[part * 16 : part * 16 + 16] + up_bias
            hidden = pre * (0.5 + 0.5 * lax.erf(pre * math.sqrt(0.5)))
            mean = jnp.mean(hidden, axis=-1, keepdims=True)
            centred = hidden - mean
            rate = lax.rsqrt(jnp.mean(centred * centred, axis=-1, keepdims=True) + EPS)
            at = pl.ds(pl.multiple_of(block * TALL + part * 16, 16), 16)
            mean_out.buffer[at] = jnp.broadcast_to(mean, (16, LANES))
            rate_out.buffer[at] = jnp.broadcast_to(rate, (16, LANES))

    mean_out.go()
    rate_out.go()
    key_code = item_codes(bounds_s, lax.broadcasted_iota(jnp.int32, (1, frames), 1))

    low = low_lanes(32)
    for block in range(frames // TALL):
        rows = pl.ds(block * TALL, TALL)
        raw = dot_nt(query_out.buffer[rows], key_out.buffer[...])
        shares = []
        for part in range(TALL // 32):
            start = block * TALL + part * 32
            index = start + lax.broadcasted_iota(jnp.int32, (32, 1), 0)
            scaled = jnp.where(
                item_codes(bounds_s, index) == key_code, raw[part * 32 : part * 32 + 32], MASKED
            )
            weight = jnp.exp(scaled - jnp.max(scaled, axis=1, keepdims=True))
            prob_out.buffer[pl.ds(start, 32)] = weight.astype(BF16)
            shares.append(1.0 / jnp.sum(weight, axis=1, keepdims=True))
        prob_out.go(rows)
        attn = dot_nn(prob_out.buffer[rows], value_out.buffer[...])
        for part in range(TALL // 32):
            share = shares[part]
            attn_out.buffer[pl.ds(block * TALL + part * 32, 32)] = jnp.where(
                low, attn[part * 32 : part * 32 + 32] * share, share
            )


def fill_margins(wide_s, frames):
    edge = jnp.zeros((MARGIN, LANES), F32)
    wide_s[:MARGIN] = edge
    wide_s[MARGIN + frames : 2 * MARGIN + frames] = edge
    base = frames + 3 * MARGIN
    after = base + frames // 2
    low = low_lanes(MARGIN)
    wide_s[base - MARGIN : base] = jnp.where(low, 0.0, turn(wide_s[after - MARGIN : after]))
    wide_s[after : after + MARGIN] = jnp.where(low, turn(wide_s[base : base + MARGIN]), 0.0)


def item_span(bounds_s, frame):
    begin, end = bounds_s[0], bounds_s[BOUNDS - 1]
    for item in range(1, ITEMS + 1):
        edge = bounds_s[item]
        begin = jnp.where(frame >= edge, edge, begin)
    for item in range(ITEMS, 0, -1):
        edge = bounds_s[item]
        end = jnp.where(frame < edge, edge, end)
    return begin, end


def is_whole(bounds_s, start):
    begin, end = item_span(bounds_s, start)
    reach = KERNEL // 2
    low = (begin == 0) | (begin <= start - reach)
    high = (end == bounds_s[BOUNDS - 1]) | (end >= start + WINDOW + reach)
    return low & high & (end >= start + WINDOW)


def tap_limits(bounds_s, start):
    frame = start + lax.broadcasted_iota(jnp.int32, (WINDOW, LANES), 0)
    begin, end = item_span(bounds_s, frame)
    return begin - frame, end - frame


def grouped(values):
    return values.reshape(WINDOW // 8, 8, LANES)


def triple_places(step, frames):
    half = frames // 2
    return (
        pl.multiple_of(step * WINDOW, 2 * MARGIN),
        pl.multiple_of(step * WINDOW + half, 2 * MARGIN),
        pl.multiple_of(step * WINDOW + frames + 2 * MARGIN, 2 * MARGIN),
    )


def over_windows(bounds_s, frames, body):
    half = frames // 2

    @pl.loop(0, half // WINDOW)
    def _(step):
        start = step * WINDOW
        whole = is_whole(bounds_s, start) & is_whole(bounds_s, start + half)

        @pl.when(whole)
        def _():
            body(step, None)

        @pl.when(jnp.logical_not(whole))
        def _():
            first, second = tap_limits(bounds_s, start), tap_limits(bounds_s, start + half)
            low = low_lanes(WINDOW)
            rest = [jnp.where(low, one, other) for one, other in zip(first, second)]
            body(step, (first, second, rest))


def tap_mask(tap, limits):
    shift = tap - KERNEL // 2
    return None if limits is None else (limits[0] <= shift) & (limits[1] > shift)


def tap_view(window_ref, tap, mask):
    view = window_ref[tap + 1 : tap + 1 + WINDOW]
    return grouped(view if mask is None else jnp.where(mask, view, 0.0))


def mlp_first_kernel(
    lengths_ref,
    n_ref,
    up_ref,
    table_ref,
    mean_ref,
    rate_ref,
    cot_ref,
    merge_ref,
    down_ref,
    attn_ref,
    mixed_out,
    gate_pre_out,
    grad_out,
    rate_out,
    hat_out,
    early_out,
    vectors_out,
    lines_out,
    hat_s,
    slope_s,
    gate_s,
    hidden_s,
    gate_slope_s,
    conv_s,
    grad_s,
    out_s,
    back_s,
    branch_s,
    mix_s,
    taps_s,
    turn_s,
    tap_sum_s,
    columns_s,
    forward_s,
    backward_s,
    bounds_s,
):
    place = lax.axis_index("tm")
    frames = mix_s.shape[0]
    half = frames // 2
    blocks = frames // BLOCK
    quarters, early_rows, _ = early_out.buffer.shape
    share = early_rows // 8
    channels = quarters * share
    fill_bounds(lengths_ref, bounds_s, frames)
    for part in range(2):
        for tap in range(KERNEL):
            line = jnp.broadcast_to(table_ref[part, 8 + tap : 9 + tap], (8, LANES))
            taps_s[part, tap] = line
            turn_s[part, KERNEL - 1 - tap] = line
    tap_sum_s[...] = jnp.zeros(tap_sum_s.shape, F32)
    main, rest = table_ref[0, :8], table_ref[1, :8]
    mixed_bias = jnp.where(low_lanes(1), rest[0:1], rest[1:2])
    low = low_lanes(64)
    gate_pre_ref = gate_pre_out.buffer
    n_ref = n_ref()
    mean_ref, rate_ref = mean_ref(), rate_ref()
    begin(cot_ref, merge_ref, down_ref, attn_ref)

    def stat_rows(rows):
        return mean_ref[rows], rate_ref[rows]

    def chunk(start, base=0):
        return pl.ds(pl.multiple_of(start, 64) + base, 64)

    def conv_part(hidden, mean, rate, lines, rows, to_rows):
        hat = (hidden - mean) * rate
        hat_s[rows] = hat
        hat_out.buffer[rows] = hat.astype(BF16)
        conv_s[to_rows] = (hat * lines[2:3] + lines[3:4]).astype(BF16).astype(F32)

    @pl.loop(0, half // TALL, unroll=2)
    def _(block):
        pre = [dot_nn(n_ref[rows_of(block, TALL, base)], up_ref[...]) for base in (0, half)]
        for part in range(TALL // 64):
            inner = slice(part * 64, part * 64 + 64)
            start = block * TALL + part * 64
            mixed = []
            for values, base in zip(pre, (0, half)):
                rows = chunk(start, base)
                gate, gate_slope = gelu_parts(values[inner, :LANES] + main[0:1])
                hidden_s[rows] = gate
                gate_slope_s[rows] = gate_slope
                hidden, slope = gelu_parts(values[inner, 2 * LANES :] + main[1:2])
                mean, rate = stat_rows(rows)
                slope_s[rows] = slope * rate
                conv_part(hidden, mean, rate, main, rows, chunk(start, base + MARGIN))
                mixed.append((*gelu_parts(values[inner, LANES : 2 * LANES] + mixed_bias), mean, rate))
            (low_hidden, low_slope, low_mean, low_rate), (high_hidden, high_slope, high_mean, high_rate) = mixed
            rows = chunk(start, frames)
            hidden_s[rows] = jnp.where(low, low_hidden, turn(high_hidden))
            gate_slope_s[rows] = jnp.where(low, low_slope, turn(high_slope))
            rate = jnp.where(low, low_rate, high_rate)
            slope_s[rows] = jnp.where(low, turn(low_slope), high_slope) * rate
            conv_part(
                jnp.where(low, turn(low_hidden), high_hidden),
                jnp.where(low, low_mean, high_mean),
                rate,
                rest,
                rows,
                chunk(start, frames + 3 * MARGIN),
            )

    hat_out.go()
    fill_margins(conv_s, frames)
    tall = WINDOW + 2 * MARGIN
    outs = (0, half, frames)

    def convolve(step, limits):
        for index, base in enumerate(triple_places(step, frames)):
            forward_s[index] = conv_s[pl.ds(base, tall)]
        for index in range(3):
            own = None if limits is None else limits[index]
            total = jnp.zeros((WINDOW // 8, 8, LANES), F32)
            for tap in range(KERNEL):
                mask = tap_mask(tap, own)
                total = total + tap_view(forward_s.at[index], tap, mask) * taps_s[index // 2, tap][None]
            lines = rest if index == 2 else main
            out_s[rows_of(step, WINDOW, outs[index])] = total.reshape(WINDOW, LANES) + lines[4:5]

    over_windows(bounds_s, frames, convolve)
    cot_ref = cot_ref()
    merge_ref = merge_ref()
    down_ref = down_ref()
    attn_ref = attn_ref()
    down_ref[channels:] = jnp.zeros((2 * LANES - channels, D), BF16)
    zero = jnp.zeros((8, LANES), F32)

    def branch_part(grad_gated, rows, to_rows, sums):
        up_sum, conv_sum = sums
        gate, conv = hidden_s[rows], out_s[rows]
        gate_pre = (grad_gated * conv * gate_slope_s[rows]).astype(BF16)
        gate_pre_ref[rows] = gate_pre
        grad_conv = (grad_gated * gate).astype(BF16).astype(F32)
        grad_s[to_rows] = grad_conv
        gate_pre = gate_pre.astype(F32)
        return gate * conv, gate_pre, (up_sum + fold_rows(gate_pre), conv_sum + fold_rows(grad_conv))

    def branch_step(block, sums):
        main_sums, rest_sums = sums
        grads = []
        for base in (0, half):
            rows = rows_of(block, TALL, base)
            branch = dot_nt(cot_ref[rows], merge_ref[...]).astype(BF16)
            branch_s[rows] = branch
            grads.append(dot_nt(branch, down_ref[...]))
        for part in range(TALL // 64):
            inner = slice(part * 64, part * 64 + 64)
            start = block * TALL + part * 64
            for values, base in zip(grads, (0, half)):
                rows = chunk(start, base)
                gated, gate_pre, main_sums = branch_part(
                    values[inner, :LANES], rows, chunk(start, base + MARGIN), main_sums
                )
                mix_s[rows, :LANES] = gated.astype(BF16)
                gate_s[rows, :LANES] = gate_pre.astype(BF16)
            grad = jnp.where(low, grads[0][inner, LANES:], turn(grads[1][inner, LANES:]))
            gated, gate_pre, rest_sums = branch_part(
                grad, chunk(start, frames), chunk(start, frames + 3 * MARGIN), rest_sums
            )
            low_rows, high_rows = chunk(start), chunk(start, half)
            gate_s[low_rows, LANES:] = gate_pre.astype(BF16)
            gate_s[high_rows, LANES:] = turn(gate_pre).astype(BF16)
            mix_s[low_rows, LANES:] = jnp.where(low, gated, turn(attn_ref[low_rows])).astype(BF16)
            mix_s[high_rows, LANES:] = jnp.where(low, turn(gated), turn(attn_ref[high_rows])).astype(BF16)
        return main_sums, rest_sums

    (main_up, main_conv), (rest_up, rest_conv) = lax.fori_loop(
        0, half // TALL, branch_step, ((zero, zero), (zero, zero)), unroll=2
    )
    gate_pre_out.go()
    fill_margins(grad_s, frames)
    own = rows_of(place, BLOCK)
    lines_out[0:1] = one_row(fold_rows(branch_s[own].astype(F32)))
    lines_out[1:2] = one_row(fold_rows(cot_ref[own].astype(F32)))
    lines_out[2:8] = jnp.zeros((6, D), F32)
    grad_down = dot_tn(mix_s[...], branch_s[...])
    grad_gate = dot_tn(gate_s[...], n_ref[...])
    for quarter in range(quarters):
        for tile in range(4):
            early_out.buffer[quarter, tile * share : (tile + 1) * share] = grad_down[
                quarter * share : (quarter + 1) * share, tile * LANES : (tile + 1) * LANES
            ].astype(BF16)
        early_out.buffer[quarter, 4 * share :] = grad_gate[
            :channels, quarter * LANES : (quarter + 1) * LANES
        ].astype(BF16)
    early_out.go()
    for block in range(blocks):
        mixed_out.buffer[block, :BLOCK] = mix_s[block * BLOCK : (block + 1) * BLOCK]
    mixed_out.go(slice(None), pl.ds(0, BLOCK))

    def differentiate(step, limits):
        for index, base in enumerate(triple_places(step, frames)):
            forward_s[index] = conv_s[pl.ds(base, tall)]
            backward_s[index] = grad_s[pl.ds(base, tall)]
        for index in range(3):
            own = None if limits is None else limits[index]
            total = jnp.zeros((WINDOW // 8, 8, LANES), F32)
            centre = grouped(backward_s[index, MARGIN : MARGIN + WINDOW])
            for tap in range(KERNEL):
                mask = tap_mask(tap, own)
                total = total + tap_view(backward_s.at[index], tap, mask) * turn_s[index // 2, tap][None]
                tap_sum_s[index // 2, tap] += jnp.sum(tap_view(forward_s.at[index], tap, mask) * centre, axis=0)
            back_s[rows_of(step, WINDOW, outs[index])] = total.reshape(WINDOW, LANES)

    over_windows(bounds_s, frames, differentiate)
    lane = lax.broadcasted_iota(jnp.int32, (64, LANES), 1)

    def norm_part(rows, lines, sums):
        gain_sum, bias_sum = sums
        back, hat, slope = back_s[rows], hat_s[rows], slope_s[rows]
        grad = back * lines[2:3]
        grad_out.buffer[rows] = (grad * slope).astype(BF16)
        rate_out.buffer[rows] = slope.astype(BF16)
        along = back * hat
        return grad, along * lines[2:3], (gain_sum + fold_rows(along), bias_sum + fold_rows(back))

    def norm_step(block, sums):
        main_sums, rest_sums = sums
        for part in range(TALL // 64):
            start = block * TALL + part * 64
            pairs = []
            for base in (0, half):
                plain, along, main_sums = norm_part(chunk(start, base), main, main_sums)
                pairs.append([plain, along])
            plain, along, rest_sums = norm_part(chunk(start, frames), rest, rest_sums)
            for item, values in enumerate((plain, along)):
                pairs[0][item] = pairs[0][item] + jnp.where(low, values, 0.0)
                pairs[1][item] = pairs[1][item] + jnp.where(low, 0.0, values)
            for (plain, along), base in zip(pairs, (0, half)):
                columns_s[chunk(start, base)] = jnp.where(
                    lane == 0,
                    jnp.sum(plain, axis=-1, keepdims=True),
                    jnp.where(lane == 1, jnp.sum(along, axis=-1, keepdims=True), 0.0),
                )
        return main_sums, rest_sums

    (main_gain, main_bias), (rest_gain, rest_bias) = lax.fori_loop(
        0, half // TALL, norm_step, ((zero, zero), (zero, zero)), unroll=2
    )
    grad_out.go()
    rate_out.go()
    totals = jnp.concatenate(
        [jnp.transpose(columns_s[block * BLOCK : (block + 1) * BLOCK])[:2] for block in range(blocks)], axis=0
    )
    high = totals.astype(BF16)
    low_part = (totals - high.astype(F32)).astype(BF16)
    for block in range(blocks):
        mixed_out.buffer[block, BLOCK:, :LANES] = high
        mixed_out.buffer[block, BLOCK:, LANES:] = low_part
    mixed_out.go(slice(None), pl.ds(BLOCK, 2 * blocks))

    def vectors(part, lines):
        taps = jnp.sum(tap_sum_s[part], axis=1)[:KERNEL]
        stacked = jnp.concatenate([taps] + [one_row(line) for line in lines], axis=0)
        if part:
            stacked = stacked + turn(stacked)
        return jnp.transpose(
            jnp.concatenate([stacked, jnp.zeros((LANES - stacked.shape[0], LANES), F32)], axis=0)
        )

    vectors_out[:LANES] = vectors(0, (main_conv, main_gain, main_bias, main_up))
    vectors_out[LANES:] = vectors(1, (rest_conv, rest_gain, rest_bias, rest_up))[: channels - LANES]


def attend_back_kernel(
    cot_ref,
    merge_ref,
    head_ref,
    attn_ref,
    value_ref,
    prob_ref,
    key_ref,
    coarse_ref,
    fine_ref,
    pos_ref,
    query_ref,
    n_ref,
    q_position_ref,
    qkv_ref,
    hat_ref,
    gain_ref,
    early_ref,
    branch_out,
    total_out,
    pack_0,
    pack_1,
    pack_2,
    pack_3,
    lines_out,
    grad_s,
    raw_s,
    projected_s,
    parts_s,
    grads_s,
):
    place = lax.axis_index("tm")
    frames = raw_s.shape[0]
    blocks = frames // BLOCK
    half = D // 2
    zero = jnp.zeros((8, LANES), F32)
    cot_ref, merge_ref, head_ref, attn_ref = cot_ref(), merge_ref(), head_ref(), attn_ref()
    head_ref[HEAD:] = jnp.zeros((LANES - HEAD, D), BF16)
    begin(value_ref, prob_ref, key_ref, pos_ref)

    @pl.loop(0, frames // TALL, unroll=4)
    def _(block):
        rows = rows_of(block, TALL)
        branch = dot_nt(cot_ref[rows], merge_ref[...]).astype(BF16)
        branch_out.buffer[rows] = branch
        grad_s[rows] = (dot_nt(branch, head_ref[...]) * attn_ref[rows, HEAD : HEAD + 1]).astype(BF16)

    branch_out.go()
    value_ref, prob_ref = value_ref(), prob_ref()
    key_ref, pos_ref = key_ref(), pos_ref()
    begin(query_ref, n_ref, q_position_ref, qkv_ref, hat_ref, early_ref)

    def score_step(block, sums):
        content_sum, position_sum = sums
        rows = rows_of(block, TALL)
        grad = grad_s[rows]
        score = dot_nt(grad, value_ref[...])
        for part in range(TALL // 32):
            at = pl.ds(pl.multiple_of(block * TALL + part * 32, 32), 32)
            inner = slice(part * 32, part * 32 + 32)
            delta = jnp.sum(grad[inner].astype(F32) * attn_ref[at], axis=1, keepdims=True)
            raw_s[at] = (prob_ref[at].astype(F32) * (score[inner] - delta)).astype(BF16)
        query = dot_nn(raw_s[rows], key_ref[...]) * 0.125
        for part in range(TALL // 32):
            at = pl.ds(pl.multiple_of(block * TALL + part * 32, 32), 32)
            inner = part * 32 % BLOCK
            sine, cosine = angle_rows(
                coarse_ref, fine_ref, block * (TALL // BLOCK) + part * 32 // BLOCK, slice(inner, inner + 32)
            )
            inner = slice(part * 32, part * 32 + 32)
            first, second = query[inner, LANES : LANES + half], query[inner, LANES + half :]
            projected_s[at, :half] = (first * sine - second * cosine).astype(BF16)
            projected_s[at, half:] = (first * cosine + second * sine).astype(BF16)
        position = dot_nn(projected_s[rows], pos_ref[...])
        content = query[:, :LANES]
        parts_s[rows, :LANES] = (content + position).astype(BF16)
        return content_sum + fold_rows(content), position_sum + fold_rows(position)

    content_sum, position_sum = lax.fori_loop(0, frames // TALL, score_step, (zero, zero), unroll=4)
    query_ref, n_ref, q_position_ref = query_ref(), n_ref(), q_position_ref()
    qkv_ref, hat_ref = qkv_ref(), hat_ref()
    grad_key = dot_tn(query_ref[...], raw_s[...])
    grad_value = dot_tn(grad_s[...], prob_ref[...])
    for block in range(blocks):
        at = slice(block * BLOCK, (block + 1) * BLOCK)
        parts_s[at, LANES : 2 * LANES] = jnp.transpose(grad_key[:, at]).astype(BF16)
        parts_s[at, 2 * LANES :] = jnp.transpose(grad_value[:, at]).astype(BF16)
    grads_s[:HEAD] = dot_tn(parts_s[:, :LANES], n_ref[...])[:HEAD]
    grads_s[HEAD : 2 * HEAD] = dot_nn(grad_key.astype(BF16), n_ref[...])[:HEAD]
    grads_s[2 * HEAD : 3 * HEAD] = dot_nn(grad_value.astype(BF16), n_ref[...])[:HEAD]
    grads_s[3 * HEAD :] = dot_tn(q_position_ref[...], projected_s[...])[:HEAD]
    stream = lax.axis_index("stream")
    early_ref = early_ref()
    for apart, pack_out in enumerate((pack_0, pack_1, pack_2, pack_3)):
        quarter = lax.bitwise_xor(stream, jnp.int32(apart))
        lanes = pl.ds(pl.multiple_of(quarter * LANES, LANES), LANES)
        pack_out.buffer[: 4 * HEAD] = grads_s[:, lanes].astype(BF16)
        pack_out.buffer[4 * HEAD :] = early_ref[quarter]
        pack_out.go()
    gain = line_of(gain_ref)
    wide_zero = jnp.zeros((8, D), F32)

    def norm_step(block, sums):
        gain_sum, bias_sum = sums
        grad = dot_nt(parts_s[rows_of(block, TALL)], qkv_ref[...])
        for part in range(TALL // 32):
            at = pl.ds(pl.multiple_of(block * TALL + part * 32, 32), 32)
            own = grad[part * 32 : part * 32 + 32]
            total_out.buffer[at] = (own * gain).astype(BF16)
            gain_sum = gain_sum + fold_rows(own * hat_ref[at].astype(F32))
            bias_sum = bias_sum + fold_rows(own)
        return gain_sum, bias_sum

    gain_sum, bias_sum = lax.fori_loop(0, frames // TALL, norm_step, (wide_zero, wide_zero), unroll=4)
    lane = lax.broadcasted_iota(jnp.int32, (1, LANES), 1)

    def own_lanes(sums):
        line = one_row(sums)
        line = line + turn(line)
        tiles = [
            jnp.where(lax.div(tile * LANES + lane, HEAD) == place, line, 0.0) for tile in range(D // LANES)
        ]
        return jnp.concatenate(tiles, axis=1)

    lines_out[...] = jnp.concatenate(
        [
            one_row(gain_sum),
            one_row(bias_sum),
            own_lanes(content_sum),
            own_lanes(position_sum),
            jnp.zeros((4, D), F32),
        ],
        axis=0,
    )


def mlp_second_kernel(
    mixed_ref,
    gate_pre_ref,
    grad_ref,
    rate_ref,
    hat_ref,
    up_ref,
    norm_hat_ref,
    gain_ref,
    other_ref,
    pre_out,
    same_out,
    apart_out,
    lines_out,
    up_out,
    columns_s,
):
    place = lax.axis_index("tm")
    pre_s = pre_out.buffer
    frames = pre_s.shape[0]
    half = frames // 2
    blocks = frames // BLOCK
    totals = jnp.zeros((2 * blocks, LANES), F32)
    mixed_ref = mixed_ref()
    for source in range(mixed_ref.shape[0]):
        both = mixed_ref[source].astype(F32)
        totals = totals + (both[:, :LANES] + both[:, LANES:])
    totals = totals * (1.0 / HALF)
    high = totals.astype(BF16)
    low_part = (totals - high.astype(F32)).astype(BF16)
    both = jnp.concatenate([high, low_part], axis=0)
    lane = lax.broadcasted_iota(jnp.int32, (4 * blocks, 2 * LANES), 1) // LANES
    line = lax.broadcasted_iota(jnp.int32, (4 * blocks, 2 * LANES), 0)
    for block in range(blocks):
        chosen = (lax.rem(line, 2 * blocks) == 2 * block + lane).astype(F32).astype(BF16)
        columns_s[block * BLOCK : (block + 1) * BLOCK] = dot_tn(both, chosen)
    gate_pre_ref, grad_ref, rate_ref, hat_ref = gate_pre_ref(), grad_ref(), rate_ref(), hat_ref()
    begin(up_ref, norm_hat_ref, other_ref)
    low = low_lanes(64)
    gain = line_of(gain_ref)

    def chunk(start, base=0):
        return pl.ds(pl.multiple_of(start, 64) + base, 64)

    def pre_part(rows, table, up_sum):
        plain, along = table
        hat, rate = hat_ref[rows].astype(F32), rate_ref[rows].astype(F32)
        pre = (grad_ref[rows].astype(F32) - rate * (plain + hat * along)).astype(BF16).astype(F32)
        return pre, up_sum + fold_rows(pre)

    def pre_step(block, sums):
        main_up, rest_up = sums
        for part in range(TALL // 64):
            start = block * TALL + part * 64
            tables = []
            for base in (0, half):
                rows = chunk(start, base)
                table = [columns_s[rows, item * LANES : (item + 1) * LANES] for item in range(2)]
                tables.append(table)
                pre, main_up = pre_part(rows, table, main_up)
                pre_s[rows, :LANES] = gate_pre_ref[rows]
                pre_s[rows, 2 * LANES :] = pre.astype(BF16)
            rows = chunk(start, frames)
            table = [jnp.where(low, one, other) for one, other in zip(*tables)]
            pre, rest_up = pre_part(rows, table, rest_up)
            gate_pre = gate_pre_ref[rows].astype(F32)
            pre_s[chunk(start), LANES : 2 * LANES] = jnp.where(low, gate_pre, turn(pre)).astype(BF16)
            pre_s[chunk(start, half), LANES : 2 * LANES] = jnp.where(low, turn(gate_pre), pre).astype(BF16)
        return main_up, rest_up

    zero = jnp.zeros((8, LANES), F32)
    main_up, rest_up = lax.fori_loop(0, half // TALL, pre_step, (zero, zero), unroll=2)
    pre_out.go()
    up_ref, norm_hat_ref, other_ref = up_ref(), norm_hat_ref(), other_ref()
    wide_zero = jnp.zeros((8, D), F32)

    def norm_step(step, sums):
        gain_sum, bias_sum = sums
        grads = dot_nt(pre_s[rows_of(step, TALL)], up_ref[...])
        for part in range(TALL // BLOCK):
            block = step * (TALL // BLOCK) + part
            rows = rows_of(block, BLOCK)
            grad = grads[part * BLOCK : (part + 1) * BLOCK]
            total = (grad * gain + other_ref[rows].astype(F32)).astype(BF16)
            apart = lax.bitwise_xor(block, place)

            @pl.when(lax.rem(apart, 2) == 0)
            def _(apart=apart, total=total):
                same_out.buffer[lax.div(apart, 2)] = total

            @pl.when(lax.rem(apart, 2) == 1)
            def _(apart=apart, total=total):
                apart_out.buffer[lax.div(apart, 2)] = total

            gain_sum = gain_sum + fold_rows(grad * norm_hat_ref[rows].astype(F32))
            bias_sum = bias_sum + fold_rows(grad)
        return gain_sum, bias_sum

    gain_sum, bias_sum = lax.fori_loop(0, frames // TALL, norm_step, (wide_zero, wide_zero), unroll=2)
    apart_out.go()
    same_out.go()
    lines_out[...] = jnp.concatenate([one_row(gain_sum), one_row(bias_sum), jnp.zeros((6, D), F32)], axis=0)
    rest_line = one_row(rest_up)
    up_out[:LANES] = jnp.transpose(jnp.broadcast_to(one_row(main_up), (LANES, LANES)))
    up_out[LANES:] = jnp.transpose(jnp.broadcast_to(rest_line + turn(rest_line), (LANES, LANES)))[:LOW]


def late_pack_kernel(
    pre_ref,
    n_ref,
    joined_ref,
    branch_ref,
    cot_ref,
    vectors_ref,
    up_columns_ref,
    first_lines_ref,
    head_lines_ref,
    own_lines_ref,
    pack_out,
):
    pack_ref = pack_out.buffer
    quarters = pack_ref.shape[0]
    channels = vectors_ref.shape[0]
    share = channels // quarters
    gate_at = KERNEL + 3
    lane = lax.broadcasted_iota(jnp.int32, (share, LANES), 1)
    lines = jnp.concatenate(
        [
            head_lines_ref[0:2],
            own_lines_ref[0:2],
            head_lines_ref[2:4],
            first_lines_ref[0:2],
            jnp.zeros((8, D), F32),
        ],
        axis=0,
    )
    for quarter in range(quarters):
        table = vectors_ref[quarter * share : (quarter + 1) * share]
        for other in range(2):
            at = slice((2 * (quarter % 2) + other) * share, (2 * (quarter % 2) + other + 1) * share)
            column = vectors_ref[at, gate_at : gate_at + 1] if quarter < quarters // 2 else up_columns_ref[at, 0:1]
            table = jnp.where(lane == gate_at + other, column, table)
        pack_ref[quarter, channels : channels + share] = table.astype(BF16)
        pack_ref[quarter, channels + share : channels + share + 16] = lines[
            :, quarter * LANES : (quarter + 1) * LANES
        ].astype(BF16)
    grad_up = dot_tn(pre_ref()[...], n_ref()[...])
    for quarter in range(quarters):
        lanes = slice(quarter * LANES, (quarter + 1) * LANES)
        pack_ref[quarter, :LANES] = grad_up[LANES:, lanes].astype(BF16)
        pack_ref[quarter, LANES:channels] = grad_up[LOW:LANES, lanes].astype(BF16)
    joined_ref, cot_ref, branch_ref = joined_ref(), cot_ref(), branch_ref()
    sources, _, rows = joined_ref.shape
    merge_rows = 2 * D // sources
    head_rows = D // sources
    grad_merge = jnp.zeros((merge_rows, D), F32)
    grad_head = jnp.zeros((head_rows, D), F32)
    for source in range(sources):
        at = slice(source * rows, (source + 1) * rows)
        joined = joined_ref[source]
        grad_merge = grad_merge + dot_nn(joined[:merge_rows], cot_ref[at])
        grad_head = grad_head + dot_nn(joined[merge_rows : merge_rows + head_rows], branch_ref[at])
    for quarter in range(quarters):
        base = channels + share + 16
        for grad in (grad_merge, grad_head):
            part = grad.shape[0] // quarters
            for tile in range(4):
                pack_ref[quarter, base : base + part] = grad[
                    quarter * part : (quarter + 1) * part, tile * LANES : (tile + 1) * LANES
                ].astype(BF16)
                base += part


def output_kernel(
    x_ref, mixed_ref, head_ref, down_ref, down_bias_ref, merge_ref, merge_bias_ref, out_ref, joined_out
):
    sources = mixed_ref.shape[0]
    rows = x_ref.shape[0]
    channels = HALF // sources
    share = channels // 4
    attn_parts = []
    branch_attn = jnp.zeros((rows, D), F32)
    branch_mlp = jnp.zeros((rows, D), F32)
    for source in range(sources):
        attn = turn(mixed_ref[source, :rows, LANES:].astype(F32))[:, :HEAD].astype(BF16)
        attn_parts.append(attn)
        branch_attn = branch_attn + dot_nn(attn, head_ref[source * HEAD : (source + 1) * HEAD])
        down = jnp.concatenate(
            [down_ref[(part * sources + source) * share : (part * sources + source + 1) * share] for part in range(4)],
            axis=0,
        )
        branch_mlp = branch_mlp + dot_nn(mixed_ref[source, :rows, :channels], down)
    joined = jnp.concatenate(
        [branch_attn.astype(BF16), (branch_mlp + line_of(down_bias_ref)).astype(BF16)], axis=1
    )
    result = x_ref[...].astype(F32) + dot_nn(joined, merge_ref[...]) + line_of(merge_bias_ref)
    out_ref[...] = result.astype(BF16)
    turned = jnp.transpose(joined.astype(F32))
    heads = jnp.transpose(jnp.concatenate(attn_parts, axis=1).astype(F32))
    merge_share = turned.shape[0] // (4 * sources)
    head_share = heads.shape[0] // (4 * sources)
    used = 4 * (merge_share + head_share)
    for target in range(sources):
        for part in range(4):
            at = (part * sources + target) * merge_share
            joined_out[target, part * merge_share : (part + 1) * merge_share] = turned[
                at : at + merge_share
            ].astype(BF16)
            at = (part * sources + target) * head_share
            to = 4 * merge_share + part * head_share
            joined_out[target, to : to + head_share] = heads[at : at + head_share].astype(BF16)
        joined_out[target, used:] = jnp.zeros((joined_out.shape[1] - used, rows), BF16)


def pair_kernel(same_ref, other_ref, *out_refs):
    for slot, out_ref in enumerate(out_refs):
        out_ref[...] = (same_ref[slot].astype(F32) + other_ref[slot].astype(F32)).astype(BF16)


def frames_kernel(x_ref, cot_ref, *refs):
    total_refs, out_ref = refs[:-1], refs[-1]
    for part in range(x_ref.shape[0] // 32):
        rows = slice(part * 32, part * 32 + 32)
        inputs = x_ref[rows].astype(F32)
        mean = jnp.mean(inputs, axis=-1, keepdims=True)
        centred = inputs - mean
        rate = lax.rsqrt(jnp.mean(centred * centred, axis=-1, keepdims=True) + EPS)
        hat = centred * rate
        grad = total_refs[0][rows].astype(F32)
        for total_ref in total_refs[1:]:
            grad = grad + total_ref[rows].astype(F32)
        plain = jnp.mean(grad, axis=-1, keepdims=True)
        along = jnp.mean(grad * hat, axis=-1, keepdims=True)
        out_ref[rows] = cot_ref[rows].astype(F32) + rate * (grad - plain - hat * along)


def add_kernel(*refs):
    out_ref = refs[-1]
    first = 0
    for at in range(0, len(refs) - 1, 4):
        total = refs[at][...].astype(F32)
        for ref in refs[at + 1 : at + 4]:
            total = total + ref[...].astype(F32)
        out_ref[first : first + total.shape[0]] = total.astype(BF16)
        first += total.shape[0]


def gather_parts(near_ref, far_ref, all_s):
    place = lax.axis_index("tm")
    for apart in range(all_s.shape[0]):
        part_ref = far_ref if apart % 2 else near_ref
        all_s[lax.bitwise_xor(jnp.int32(apart), place)] = part_ref[apart // 2]


def lines_from(all_s, base, size):
    return jnp.concatenate([all_s[source, base : base + size] for source in range(all_s.shape[0])], axis=0).astype(F32)


def add_streams_kernel(parts_ref, out_ref):
    total = parts_ref[0].astype(F32)
    for source in range(1, parts_ref.shape[0]):
        total = total + parts_ref[source].astype(F32)
    out_ref[...] = total.astype(BF16)


def early_kernel(near_ref, far_ref, qkv_out, pos_out, down_out, up_out, all_s):
    gather_parts(near_ref, far_ref, all_s)
    sources = all_s.shape[0]
    share = HALF // (4 * sources)
    for kind in range(4):
        lines = jnp.transpose(lines_from(all_s, kind * HEAD, HEAD))
        if kind < 3:
            qkv_out[:, kind * D : (kind + 1) * D] = lines
        else:
            pos_out[...] = lines
    base = 4 * HEAD
    for source in range(sources):
        for tile in range(4):
            down_out[source * share : (source + 1) * share, tile * LANES : (tile + 1) * LANES] = all_s[
                source, base + tile * share : base + (tile + 1) * share
            ].astype(F32)
    wide = sources * share
    for group in range(4):
        up_out.buffer[:, group * wide : (group + 1) * wide] = jnp.transpose(
            lines_from(all_s, base + 4 * share + group * share, share)
        )


def late_kernel(*refs):
    _, near_ref, far_ref = refs[:3]
    (
        attn_gain_out,
        attn_bias_out,
        mlp_gain_out,
        mlp_bias_out,
        content_out,
        position_out,
        outw_out,
        up_out,
        up_bias_out,
        gain_out,
        bias_out,
        taps_out,
        conv_bias_out,
        down_bias_out,
        merge_out,
        merge_bias_out,
        all_s,
    ) = refs[3:]
    gather_parts(near_ref, far_ref, all_s)
    sources = all_s.shape[0]
    channels = HALF // sources
    share = channels // 4
    base = 0
    for group in range(4):
        at = group * sources * share
        up_out.buffer[:, at : at + sources * share] = jnp.transpose(lines_from(all_s, base + group * share, share))
    up_out.go()
    table = jnp.transpose(lines_from(all_s, base + channels, share))
    taps_out[...] = table[:KERNEL]
    conv_bias_out[...] = table[KERNEL]
    gain_out[...] = table[KERNEL + 1]
    bias_out[...] = table[KERNEL + 2]
    wide = sources * share
    up_bias_out[:wide] = table[KERNEL + 3]
    up_bias_out[wide:] = table[KERNEL + 4]
    base = base + channels + share
    lines = all_s[0, base : base + 16].astype(F32)
    for source in range(1, sources):
        lines = lines + all_s[source, base : base + 16].astype(F32)
    outs = (attn_gain_out, attn_bias_out, mlp_gain_out, mlp_bias_out, content_out, position_out, down_bias_out, merge_bias_out)
    for line, out in enumerate(outs):
        out[...] = lines[line]
    base = base + 16
    merge_share = 2 * D // (4 * sources)
    head_share = D // (4 * sources)
    for source in range(sources):
        for tile in range(4):
            lanes = slice(tile * LANES, (tile + 1) * LANES)
            at = base + tile * merge_share
            merge_out[source * merge_share : (source + 1) * merge_share, lanes] = all_s[
                source, at : at + merge_share
            ].astype(F32)
            at = base + 4 * merge_share + tile * head_share
            outw_out[source * head_share : (source + 1) * head_share, lanes] = all_s[
                source, at : at + head_share
            ].astype(F32)


def moved(block, axis, bits):
    count = lax.axis_size(axis)
    return lax.ppermute(block, axis, [(index, index ^ bits) for index in range(count)])


def over_streams(packs):
    return [packs[0]] + [moved(packs[bits], "stream", bits) for bits in range(1, lax.axis_size("stream"))]


def near_blocks(block):
    return [block] + [moved(block, "tm", bits) for bits in range(2, lax.axis_size("tm"), 2)]


def far_blocks(near):
    far = [moved(part, "tm", 1) for part in near]
    return [part for pair in zip(near, far) for part in pair]


def far_stack(near):
    stack = jnp.stack(near)
    return stack, moved(stack, "tm", 1)


def head_device(
    frames,
    lengths,
    cotangent,
    ln_attn_gain,
    ln_attn_bias,
    ln_mlp_gain,
    ln_mlp_bias,
    qkv_weight,
    content_bias,
    position_bias,
    pos_weight,
    out_weight,
    up_weight,
    up_bias,
    gate_norm_gain,
    gate_norm_bias,
    conv_kernel,
    conv_bias,
    down_weight,
    down_bias,
    merge_weight,
    merge_bias,
):
    count = lax.axis_size("tm")
    quarters = lax.axis_size("stream")
    own = frames.shape[1]
    total = own * count
    folded = total + total // 2
    padded = folded + 4 * MARGIN
    share = HALF // (quarters * count)
    channels = HALF // count
    quarter = D // quarters
    own_frames = frames[0]
    own_cotangent = cotangent[0]

    whole, late = Part(), Part(late=True)
    near = near_blocks(jnp.concatenate([own_frames, own_cotangent], axis=1))
    up_own, table, qkv_own, pos_own, bias_own = kernel_call(
        select_kernel,
        [
            ((D, 3 * LANES), BF16),
            ((2, 8 + KERNEL + 1, LANES), F32),
            ((D, 3 * LANES), BF16),
            ((D, LANES), BF16),
            ((8, LANES), F32),
        ],
        10 * "v",
    )(
        up_weight,
        up_bias,
        gate_norm_gain,
        gate_norm_bias,
        conv_bias,
        conv_kernel,
        qkv_weight,
        pos_weight,
        content_bias,
        position_bias,
    )
    frequency = jnp.exp(jnp.arange(D // 2, dtype=F32) * (-2.0 * math.log(10000.0) / D))
    coarse = jnp.arange(0, total, BLOCK, dtype=F32)[:, None] * frequency[None]
    fine = jnp.arange(BLOCK, dtype=F32)[:, None] * frequency[None]
    coarse_table = jnp.concatenate([jnp.sin(coarse), jnp.cos(coarse)], axis=1)
    fine_table = jnp.concatenate([jnp.sin(fine), jnp.cos(fine)], axis=1)
    near, up_own, coarse_table, fine_table = lax.optimization_barrier((near, up_own, coarse_table, fine_table))
    blocks = far_blocks(near)

    n_attn, n_mlp, hat, q_position, query, key, value, prob, attn, mean, rate = kernel_call(
        attend_kernel,
        [
            ((total, D), BF16, 1),
            ((total, D), BF16, 1),
            ((total, D), BF16, 1),
            ((total, LANES), BF16, 1),
            ((total, LANES + D), BF16, 1),
            ((total, LANES + D), BF16, 1),
            ((total, LANES), BF16, 1),
            ((total, total), BF16, 1),
            ((total, LANES), F32, 1),
            ((total, LANES), F32, 1),
            ((total, LANES), F32, 1),
        ],
        [
            "s",
            blocks_part(0),
            *"vvvvvvvvv",
            Part((D, HALF), lambda refs, buffer: [(refs[0].at[:, pl.ds(HALF, HALF)], buffer)], late=True),
            "v",
        ],
        bounds=True,
    )(
        lengths,
        *blocks,
        ln_attn_gain,
        ln_attn_bias,
        ln_mlp_gain,
        ln_mlp_bias,
        qkv_own,
        pos_own,
        bias_own,
        coarse_table,
        fine_table,
        up_weight,
        up_bias,
    )

    def own_down(refs, buffer):
        place = lax.axis_index("tm")
        stride = HALF // quarters
        return [
            (
                refs[0].at[pl.ds(pl.multiple_of(part * stride + share * place, 16), share)],
                buffer.at[pl.ds(part * share, share)],
            )
            for part in range(quarters)
        ]

    mixed, gate_pre, grad_y, slope, gate_hat, early_pack, vectors, first_lines = kernel_call(
        mlp_first_kernel,
        [
            ((count, own + 16, 2 * LANES), BF16, 1),
            ((folded, LANES), BF16, 1),
            ((folded, LANES), BF16, 1),
            ((folded, LANES), BF16, 1),
            ((folded, LANES), BF16, 1),
            ((quarters, 8 * share, LANES), BF16, 1),
            ((channels, LANES), F32),
            ((8, D), F32),
        ],
        [
            "s",
            whole,
            "v",
            "v",
            whole,
            whole,
            blocks_part(1, late=True),
            rows_part(D, D, late=True),
            Part((2 * LANES, D), own_down, late=True),
            Part(late=True),
        ],
        [
            ((folded, LANES), F32),
            ((folded, LANES), F32),
            ((total, 2 * LANES), BF16),
            ((folded, LANES), F32),
            ((folded, LANES), F32),
            ((padded, LANES), F32),
            ((padded, LANES), F32),
            ((folded, LANES), F32),
            ((folded, LANES), F32),
            ((total, D), BF16),
            ((total, 2 * LANES), BF16),
            ((2, 32, 8, LANES), F32),
            ((2, 32, 8, LANES), F32),
            ((2, 32, 8, LANES), F32),
            ((total, LANES), F32),
            ((3, WINDOW + 2 * MARGIN, LANES), F32),
            ((3, WINDOW + 2 * MARGIN, LANES), F32),
        ],
        bounds=True,
    )(lengths, n_mlp, up_own, table, mean, rate, *blocks, merge_weight, down_weight, attn)
    mixed_own = lax.all_to_all(mixed, "tm", 0, 0, tiled=True)

    def own_head(refs, buffer):
        at = pl.ds(pl.multiple_of(lax.axis_index("tm") * HEAD, HEAD), HEAD)
        return [(refs[0].at[at], buffer.at[pl.ds(0, HEAD)])]

    branch, from_attn, *head_packs, head_lines = kernel_call(
        attend_back_kernel,
        [
            ((total, D), BF16, 1),
            ((total, D), BF16, 1),
            *([((4 * HEAD + 8 * share, LANES), BF16, 1)] * quarters),
            ((8, D), F32),
        ],
        [
            blocks_part(1),
            rows_part(0, D),
            Part((LANES, D), own_head),
            whole,
            late,
            late,
            late,
            "v",
            "v",
            late,
            Part((total, LANES), lambda refs, buffer: [(refs[0].at[:, pl.ds(0, LANES)], buffer)], late=True),
            late,
            late,
            late,
            late,
            "v",
            late,
        ],
        [
            ((total, LANES), BF16),
            ((total, total), BF16),
            ((total, D), BF16),
            ((total, 3 * LANES), BF16),
            ((4 * HEAD, D), F32),
        ],
    )(
        *blocks,
        merge_weight,
        out_weight,
        attn,
        value,
        prob,
        key,
        coarse_table,
        fine_table,
        pos_own,
        query,
        n_attn,
        q_position,
        qkv_own,
        hat,
        ln_attn_gain,
        early_pack,
    )
    head_parts = over_streams(head_packs)
    mixed_own, _ = lax.optimization_barrier((mixed_own, head_lines))
    out_rows, joined = kernel_call(
        output_kernel,
        [((own, D), BF16), ((count, 256, own), BF16)],
        "vvvvvvv",
        megas=24,
    )(own_frames, mixed_own, out_weight, down_weight, down_bias, merge_weight, merge_bias)
    joined_all = lax.all_to_all(joined, "tm", 0, 0, tiled=True)
    gate_pre, _ = lax.optimization_barrier((gate_pre, joined))
    late_rows = 5 * share + 16 + 3 * D // count
    pre, same, apart, own_lines, up_columns = kernel_call(
        mlp_second_kernel,
        [
            ((total, 3 * LANES), BF16, 1),
            ((count // 2, own, D), BF16, 1),
            ((count // 2, own, D), BF16, 1),
            ((8, D), F32),
            ((channels, LANES), F32),
        ],
        [
            Part(
                (count, 2 * total // BLOCK, 2 * LANES),
                lambda refs, buffer: [(refs[0].at[:, pl.ds(own, 2 * total // BLOCK)], buffer)],
            ),
            *([whole] * 4),
            late,
            late,
            "v",
            late,
        ],
        [((total, 2 * LANES), F32)],
    )(mixed_own, gate_pre, grad_y, slope, gate_hat, up_own, hat, ln_mlp_gain, from_attn)
    sibling = moved(apart, "tm", 1)
    pre, joined_all = lax.optimization_barrier((pre, joined_all))
    (late_pack,) = kernel_call(
        late_pack_kernel,
        [((quarters, late_rows, LANES), BF16, 1)],
        [
            Part(
                (total, 2 * LANES),
                lambda refs, buffer: [(refs[0].at[:, pl.ds(LANES, 2 * LANES)], buffer)],
            ),
            whole,
            whole,
            whole,
            blocks_part(1),
            *"vvvvv",
        ],
    )(pre, n_mlp, joined_all, branch, *blocks, vectors, up_columns, first_lines, head_lines, own_lines)
    late_pack, head_parts = lax.optimization_barrier((late_pack, head_parts))
    late_moved = lax.all_to_all(late_pack, "stream", 0, 0, tiled=True)
    (early_part,) = kernel_call(add_kernel, [((4 * HEAD + 8 * share, LANES), BF16)], quarters * "v", megas=24)(
        *head_parts
    )
    early_near = near_blocks(early_part)
    pairs = kernel_call(pair_kernel, [((own, D), BF16)] * (count // 2), "vv", megas=24)(same, sibling)
    late_moved, early_near, pairs = lax.optimization_barrier((late_moved, early_near, pairs))
    sums = [pairs[0]] + [moved(pairs[slot], "tm", 2 * slot) for slot in range(1, count // 2)]
    (late_part,) = kernel_call(add_streams_kernel, [((late_rows, LANES), BF16)], "v", megas=24)(late_moved)
    late_near = near_blocks(late_part)
    early_all = far_stack(early_near)
    grad_qkv, grad_pos, grad_down, half_up = kernel_call(
        early_kernel,
        [
            ((quarter, 3 * D), F32),
            ((quarter, D), F32),
            ((HALF // quarters, D), F32),
            ((quarter, 2 * HALF), F32, 1, (quarter, HALF), lambda ref: ref.at[:, pl.ds(0, HALF)]),
        ],
        "vv",
        [((count, 4 * HEAD + 8 * share, LANES), BF16)],
        megas=24,
    )(*early_all)
    late_near, grad_pos, sums = lax.optimization_barrier((late_near, grad_pos, sums))
    late_parts = far_stack(late_near)
    (grad_frames,) = kernel_call(frames_kernel, [((own, D), F32)], (2 + count // 2) * "v", megas=24)(
        own_frames, own_cotangent, *sums
    )
    late_parts, grad_frames = lax.optimization_barrier((late_parts, grad_frames))
    late = kernel_call(
        late_kernel,
        [((quarter,), F32)] * 6
        + [
            ((quarter, D), F32),
            ((quarter, 2 * HALF), F32, 1, (quarter, HALF), lambda ref: ref.at[:, pl.ds(HALF, HALF)]),
            ((2 * HALF // quarters,), F32),
            ((HALF // quarters,), F32),
            ((HALF // quarters,), F32),
            ((KERNEL, HALF // quarters), F32),
            ((HALF // quarters,), F32),
            ((quarter,), F32),
            ((2 * D // quarters, D), F32),
            ((quarter,), F32),
        ],
        "kvv",
        [((count,) + late_part.shape, BF16)],
        megas=24,
        aliases={0: 7},
    )(half_up, *late_parts)
    return (
        out_rows[None],
        grad_frames[None],
        *late[:4],
        grad_qkv,
        *late[4:6],
        grad_pos,
        *late[6:13],
        grad_down,
        *late[13:],
    )


def per_device(*operands):
    fits = (
        lax.axis_size("tm") == HEADS
        and lax.axis_size("stream") * LANES == D
        and operands[0].shape[1] == BLOCK
    )
    return head_device(*operands) if fits else frame_device(*operands)


def solution(mesh):
    return jax.shard_map(
        per_device,
        mesh=mesh,
        in_specs=(
            P("stream", "tm", None),
            P("stream", None),
            P("stream", "tm", None),
            P(),
            P(),
            P(),
            P(),
            P(),
            P(),
            P(),
            P(),
            P(),
            P(),
            P(),
            P(),
            P(),
            P(),
            P(),
            P(),
            P(),
            P(),
            P(),
        ),
        out_specs=(
            P("stream", "tm", None),
            P("stream", "tm", None),
            P("stream"),
            P("stream"),
            P("stream"),
            P("stream"),
            P("stream", None),
            P("stream"),
            P("stream"),
            P("stream", None),
            P("stream", None),
            P("stream", None),
            P("stream"),
            P("stream"),
            P("stream"),
            P(None, "stream"),
            P("stream"),
            P("stream", None),
            P("stream"),
            P("stream", None),
            P("stream"),
        ),
        check_vma=False,
    )
```

```python
import math

import jax
import jax.numpy as jnp
from jax import lax
from jax.experimental import pallas as pl
from jax.experimental.pallas import tpu as pltpu
from jax.sharding import PartitionSpec as P

D = 512
HEADS = 8
HEAD = 64
KERNEL = 31
ITEMS = 5
HALF = 1536


EPS = 1e-05
MASKED = -1e30


def extended(block, sides, width):
    for axis, dim in sides:
        count = lax.axis_size(axis)
        forward = [(i, i + 1) for i in range(count - 1)]
        backward = [(target, source) for source, target in forward]
        low = lax.ppermute(
            lax.slice_in_dim(block, block.shape[dim] - width, None, axis=dim), axis, forward
        )
        high = lax.ppermute(lax.slice_in_dim(block, 0, width, axis=dim), axis, backward)
        block = jnp.concatenate([low, block, high], axis=dim)
    return block


def norm_rows(inputs, scale_row, shift_row):
    row_mean = jnp.mean(inputs, axis=-1, keepdims=True)
    centred = inputs - row_mean
    spread = jnp.mean(centred * centred, axis=-1, keepdims=True)
    return centred * lax.rsqrt(spread + EPS) * scale_row + shift_row


def gelu_exact(inputs):
    return jax.nn.gelu(inputs, approximate=False)


def frame_info(lengths, offset, extent):
    item_ends = jnp.cumsum(lengths)
    first_table = jnp.concatenate([item_ends - lengths, item_ends[-1:]])
    frame_index = offset + jnp.arange(extent, dtype=jnp.int32)
    item_of = jnp.sum((frame_index[:, None] >= item_ends[None, :]).astype(jnp.int32), axis=1)
    labels = jnp.arange(ITEMS + 1, dtype=jnp.int32)
    first_frame = jnp.sum(
        jnp.where(item_of[:, None] == labels[None, :], first_table[None, :], 0), axis=1
    )
    return (frame_index, item_of, frame_index - first_frame)


def angles(place_in):
    frequency = jnp.exp(jnp.arange(D // 2, dtype=jnp.float32) * (-2.0 * math.log(10000.0) / D))
    phase_angle = place_in.astype(jnp.float32)[:, None] * frequency[None, :]
    return (jnp.sin(phase_angle), jnp.cos(phase_angle))


def rel_query(projected, sine_rows, cosine_rows):
    half_size = projected.shape[-1] // 2
    first_half = projected[..., :half_size]
    second_half = projected[..., half_size:]
    sine_wide = sine_rows[:, None, :]
    cosine_wide = cosine_rows[:, None, :]
    return jnp.concatenate(
        [
            first_half * sine_wide + second_half * cosine_wide,
            second_half * sine_wide - first_half * cosine_wide,
        ],
        axis=-1,
    )


def step_size(extent):
    return math.gcd(extent, 512)


def score_block(q_content, q_rel, query_item, query_frame, key_block, key_start, lengths):
    extent = key_block.shape[0]
    key_frame, key_item, key_place = frame_info(lengths, key_start, extent)
    sine_rows, cosine_rows = angles(key_place)
    k_rel = jnp.concatenate([cosine_rows, sine_rows], axis=1).astype(jnp.bfloat16)
    raw_scores = jnp.einsum(
        "qhe,khe->hqk",
        q_content,
        key_block.reshape(extent, HEADS, HEAD),
        preferred_element_type=jnp.float32,
    )
    raw_scores = raw_scores + jnp.einsum(
        "qhc,kc->hqk", q_rel, k_rel, preferred_element_type=jnp.float32
    )
    allowed = (query_item[:, None] == key_item[None, :]) & (
        (query_item[:, None] < ITEMS) | (query_frame[:, None] == key_frame[None, :])
    )
    return (raw_scores, allowed, k_rel)


def block_grads(
    q_content,
    q_rel,
    query_item,
    query_frame,
    grad_out,
    log_total,
    delta_rows,
    key_block,
    value_block,
    key_start,
    lengths,
):
    extent = key_block.shape[0]
    raw_scores, allowed, k_rel = score_block(
        q_content, q_rel, query_item, query_frame, key_block, key_start, lengths
    )
    prob_rows = jnp.where(allowed[None], jnp.exp(raw_scores * 0.125 - log_total[:, :, None]), 0.0)
    grad_prob = jnp.einsum(
        "qhe,khe->hqk",
        grad_out,
        value_block.reshape(extent, HEADS, HEAD),
        preferred_element_type=jnp.float32,
    )
    grad_raw = (prob_rows * (grad_prob - delta_rows[:, :, None]) * 0.125).astype(jnp.bfloat16)
    return (prob_rows.astype(jnp.bfloat16), grad_raw, k_rel)


def frame_device(
    frames,
    lengths,
    cotangent,
    ln_attn_gain,
    ln_attn_bias,
    ln_mlp_gain,
    ln_mlp_bias,
    qkv_weight,
    content_bias,
    position_bias,
    pos_weight,
    out_weight,
    up_weight,
    up_bias,
    gate_norm_gain,
    gate_norm_bias,
    conv_kernel,
    conv_bias,
    down_weight,
    down_bias,
    merge_weight,
    merge_bias,
):
    row_count = frames.shape[1]
    cycle_size = lax.axis_size("tm")
    offset = lax.axis_index("tm") * row_count
    stream_lengths = lengths[0]
    inputs = frames[0].astype(jnp.float32)
    frame_index, item_of, place_in = frame_info(stream_lengths, offset, row_count)
    sine_rows, cosine_rows = angles(place_in)
    attn_norm, attn_pull = jax.vjp(
        norm_rows, inputs, ln_attn_gain.astype(jnp.float32), ln_attn_bias.astype(jnp.float32)
    )
    mlp_norm, mlp_pull = jax.vjp(
        norm_rows, inputs, ln_mlp_gain.astype(jnp.float32), ln_mlp_bias.astype(jnp.float32)
    )
    attn_norm_low = attn_norm.astype(jnp.bfloat16)
    mlp_norm_low = mlp_norm.astype(jnp.bfloat16)
    qkv_rows = jnp.dot(attn_norm_low, qkv_weight, preferred_element_type=jnp.float32)
    query_rows = qkv_rows[:, :D]
    key_rows = qkv_rows[:, D : 2 * D].astype(jnp.bfloat16)
    value_rows = qkv_rows[:, 2 * D :].astype(jnp.bfloat16)
    q_content = (query_rows + content_bias.astype(jnp.float32)).astype(jnp.bfloat16)
    q_position = (query_rows + position_bias.astype(jnp.float32)).astype(jnp.bfloat16)
    content_heads = q_content.reshape(row_count, HEADS, HEAD)
    position_heads = q_position.reshape(row_count, HEADS, HEAD)
    pos_heads = pos_weight.reshape(D, HEADS, HEAD)
    projected = jnp.einsum(
        "the,che->thc", position_heads, pos_heads, preferred_element_type=jnp.float32
    )
    q_rel = rel_query(projected, sine_rows, cosine_rows).astype(jnp.bfloat16)
    start_state = (
        jnp.full((HEADS, row_count), MASKED, jnp.float32),
        jnp.zeros((HEADS, row_count), jnp.float32),
        jnp.zeros((HEADS, row_count, HEAD), jnp.float32),
    )
    fold_state = start_state
    key_piece = lax.all_gather(key_rows, "tm", axis=0, tiled=True)
    value_piece = lax.all_gather(value_rows, "tm", axis=0, tiled=True)
    extent = key_piece.shape[0]
    step_rows = step_size(extent)

    def forward_one_step(inner_state, step_index):
        row_top, row_total, row_acc = inner_state
        key_block = lax.dynamic_slice_in_dim(key_piece, step_index * step_rows, step_rows, 0)
        value_block = lax.dynamic_slice_in_dim(value_piece, step_index * step_rows, step_rows, 0)
        raw_scores, allowed, k_rel = score_block(
            content_heads,
            q_rel,
            item_of,
            frame_index,
            key_block,
            step_index * step_rows,
            stream_lengths,
        )
        scaled = jnp.where(allowed[None], raw_scores * 0.125, MASKED)
        new_top = jnp.maximum(row_top, jnp.max(scaled, axis=2))
        weight = jnp.where(allowed[None], jnp.exp(scaled - new_top[:, :, None]), 0.0)
        factor = jnp.exp(row_top - new_top)
        row_total = row_total * factor + jnp.sum(weight, axis=2)
        row_acc = row_acc * factor[:, :, None] + jnp.einsum(
            "hqk,khe->hqe",
            weight.astype(jnp.bfloat16),
            value_block.reshape(step_rows, HEADS, HEAD),
            preferred_element_type=jnp.float32,
        )
        return ((new_top, row_total, row_acc), None)

    fold_state, unused = lax.scan(
        forward_one_step, fold_state, jnp.arange(extent // step_rows, dtype=jnp.int32)
    )
    row_top, row_total, row_acc = fold_state
    attn_heads = row_acc / row_total[:, :, None]
    log_total = row_top + jnp.log(row_total)
    attn_low = jnp.transpose(attn_heads, (1, 0, 2)).reshape(row_count, D).astype(jnp.bfloat16)
    branch_attn = jnp.dot(attn_low, out_weight, preferred_element_type=jnp.float32).astype(
        jnp.bfloat16
    )
    hidden_pre = jnp.dot(
        mlp_norm_low, up_weight, preferred_element_type=jnp.float32
    ) + up_bias.astype(jnp.float32)
    hidden, gelu_pull = jax.vjp(gelu_exact, hidden_pre)
    gate_half = hidden[:, :HALF]
    conv_norm, conv_pull = jax.vjp(
        norm_rows,
        hidden[:, HALF:],
        gate_norm_gain.astype(jnp.float32),
        gate_norm_bias.astype(jnp.float32),
    )
    conv_in = conv_norm.astype(jnp.bfloat16)
    half_width = KERNEL // 2
    conv_wide = extended(conv_in, (("tm", 0),), half_width)
    wide_frame, wide_item, wide_place = frame_info(
        stream_lengths, offset - half_width, row_count + 2 * half_width
    )
    kernel_rows = conv_kernel.astype(jnp.float32)
    conv_out = conv_bias.astype(jnp.float32) + jnp.zeros_like(gate_half)
    for tap_index in range(KERNEL):
        same_item = (wide_item[tap_index : tap_index + row_count] == item_of)[:, None]
        conv_out = (
            conv_out
            + jnp.where(
                same_item, conv_wide[tap_index : tap_index + row_count].astype(jnp.float32), 0.0
            )
            * kernel_rows[tap_index]
        )
    gated_low = (gate_half * conv_out).astype(jnp.bfloat16)
    branch_mlp = (
        jnp.dot(gated_low, down_weight, preferred_element_type=jnp.float32)
        + down_bias.astype(jnp.float32)
    ).astype(jnp.bfloat16)
    joined = jnp.concatenate([branch_attn, branch_mlp], axis=1)
    result = (
        inputs
        + jnp.dot(joined, merge_weight, preferred_element_type=jnp.float32)
        + merge_bias.astype(jnp.float32)
    )
    out_rows = result.astype(jnp.bfloat16)[None]
    grad_low = cotangent[0]
    grad_rows = grad_low.astype(jnp.float32)
    grad_merge_bias = jnp.sum(grad_rows, axis=0)
    grad_merge_weight = jnp.einsum(
        "tc,td->cd", joined, grad_low, preferred_element_type=jnp.float32
    )
    grad_joined = jnp.einsum(
        "td,cd->tc", grad_low, merge_weight, preferred_element_type=jnp.float32
    )
    grad_attn_branch = grad_joined[:, :D].astype(jnp.bfloat16)
    grad_mlp_branch = grad_joined[:, D:].astype(jnp.bfloat16)
    grad_down_weight = jnp.einsum(
        "tc,td->cd", gated_low, grad_mlp_branch, preferred_element_type=jnp.float32
    )
    grad_down_bias = jnp.sum(grad_mlp_branch.astype(jnp.float32), axis=0)
    grad_gated = jnp.einsum(
        "td,cd->tc", grad_mlp_branch, down_weight, preferred_element_type=jnp.float32
    )
    grad_gate_half = grad_gated * conv_out
    grad_conv_out = (grad_gated * gate_half).astype(jnp.bfloat16)
    grad_conv_rows = grad_conv_out.astype(jnp.float32)
    grad_conv_bias = jnp.sum(grad_conv_rows, axis=0)
    grad_wide = extended(grad_conv_out, (("tm", 0),), half_width)
    kernel_list = []
    grad_conv_in = jnp.zeros_like(grad_conv_rows)
    for tap_index in range(KERNEL):
        same_item = (wide_item[tap_index : tap_index + row_count] == item_of)[:, None]
        kernel_list.append(
            jnp.sum(
                jnp.where(
                    same_item, conv_wide[tap_index : tap_index + row_count].astype(jnp.float32), 0.0
                )
                * grad_conv_rows,
                axis=0,
            )
        )
        back_start = 2 * half_width - tap_index
        back_item = (wide_item[back_start : back_start + row_count] == item_of)[:, None]
        grad_conv_in = (
            grad_conv_in
            + jnp.where(
                back_item, grad_wide[back_start : back_start + row_count].astype(jnp.float32), 0.0
            )
            * kernel_rows[tap_index]
        )
    grad_conv_kernel = jnp.stack(kernel_list)
    grad_second, grad_gate_norm_gain, grad_gate_norm_bias = conv_pull(grad_conv_in)
    (grad_pre_rows,) = gelu_pull(jnp.concatenate([grad_gate_half, grad_second], axis=1))
    grad_pre = grad_pre_rows.astype(jnp.bfloat16)
    grad_up_bias = jnp.sum(grad_pre.astype(jnp.float32), axis=0)
    grad_up_weight = jnp.einsum(
        "tc,tf->cf", mlp_norm_low, grad_pre, preferred_element_type=jnp.float32
    )
    grad_mlp_norm = jnp.einsum("tf,cf->tc", grad_pre, up_weight, preferred_element_type=jnp.float32)
    grad_out_weight = jnp.einsum(
        "tc,td->cd", attn_low, grad_attn_branch, preferred_element_type=jnp.float32
    )
    grad_attn_low = jnp.einsum(
        "td,cd->tc", grad_attn_branch, out_weight, preferred_element_type=jnp.float32
    ).astype(jnp.bfloat16)
    grad_out_heads = grad_attn_low.reshape(row_count, HEADS, HEAD)
    delta_rows = jnp.sum(
        jnp.transpose(grad_out_heads.astype(jnp.float32), (1, 0, 2)) * attn_heads, axis=2
    )
    total_frames = row_count * cycle_size
    back_start_state = (
        jnp.zeros((row_count, HEADS, HEAD), jnp.float32),
        jnp.zeros((row_count, HEADS, D), jnp.float32),
        jnp.zeros((total_frames, D), jnp.float32),
        jnp.zeros((total_frames, D), jnp.float32),
    )
    back_key_piece = lax.all_gather(key_rows, "tm", axis=0, tiled=True)
    back_value_piece = lax.all_gather(value_rows, "tm", axis=0, tiled=True)
    extent = back_key_piece.shape[0]
    back_step_rows = step_size(extent)

    def back_one_step(inner_state, step_index):
        grad_content, grad_rel = inner_state
        key_block = lax.dynamic_slice_in_dim(
            back_key_piece, step_index * back_step_rows, back_step_rows, 0
        )
        value_block = lax.dynamic_slice_in_dim(
            back_value_piece, step_index * back_step_rows, back_step_rows, 0
        )
        prob_low, grad_raw, k_rel = block_grads(
            content_heads,
            q_rel,
            item_of,
            frame_index,
            grad_out_heads,
            log_total,
            delta_rows,
            key_block,
            value_block,
            step_index * back_step_rows,
            stream_lengths,
        )
        grad_content = grad_content + jnp.einsum(
            "hqk,khe->qhe",
            grad_raw,
            key_block.reshape(back_step_rows, HEADS, HEAD),
            preferred_element_type=jnp.float32,
        )
        grad_rel = grad_rel + jnp.einsum(
            "hqk,kc->qhc", grad_raw, k_rel, preferred_element_type=jnp.float32
        )
        key_part = jnp.einsum(
            "hqk,qhe->khe", grad_raw, content_heads, preferred_element_type=jnp.float32
        ).reshape(back_step_rows, D)
        value_part = jnp.einsum(
            "hqk,qhe->khe", prob_low, grad_out_heads, preferred_element_type=jnp.float32
        ).reshape(back_step_rows, D)
        return ((grad_content, grad_rel), (key_part, value_part))

    inner_state, block_parts = lax.scan(
        back_one_step,
        (back_start_state[0], back_start_state[1]),
        jnp.arange(extent // back_step_rows, dtype=jnp.int32),
    )
    key_all = block_parts[0].reshape(extent, D)
    value_all = block_parts[1].reshape(extent, D)
    grad_content, grad_rel, key_all, value_all = (
        inner_state[0],
        inner_state[1],
        key_all,
        value_all,
    )
    grad_keys, grad_values = (
        lax.psum_scatter(key_all, "tm", scatter_dimension=0, tiled=True),
        lax.psum_scatter(value_all, "tm", scatter_dimension=0, tiled=True),
    )
    half_size = D // 2
    rel_first = grad_rel[..., :half_size]
    rel_second = grad_rel[..., half_size:]
    sine_wide = sine_rows[:, None, :]
    cosine_wide = cosine_rows[:, None, :]
    grad_projected = jnp.concatenate(
        [
            rel_first * sine_wide - rel_second * cosine_wide,
            rel_first * cosine_wide + rel_second * sine_wide,
        ],
        axis=-1,
    ).astype(jnp.bfloat16)
    grad_pos_weight = jnp.einsum(
        "thc,the->che", grad_projected, position_heads, preferred_element_type=jnp.float32
    ).reshape(D, D)
    grad_q_position = jnp.einsum(
        "thc,che->the", grad_projected, pos_heads, preferred_element_type=jnp.float32
    )
    grad_content_bias = jnp.sum(grad_content, axis=0).reshape(D)
    grad_position_bias = jnp.sum(grad_q_position, axis=0).reshape(D)
    grad_query = (grad_content + grad_q_position).reshape(row_count, D).astype(jnp.bfloat16)
    grad_qkv = jnp.concatenate(
        [grad_query, grad_keys.astype(jnp.bfloat16), grad_values.astype(jnp.bfloat16)], axis=1
    )
    grad_qkv_weight = jnp.einsum(
        "tc,tf->cf", attn_norm_low, grad_qkv, preferred_element_type=jnp.float32
    )
    grad_attn_norm = jnp.einsum(
        "tf,cf->tc", grad_qkv, qkv_weight, preferred_element_type=jnp.float32
    )
    grad_from_attn, grad_ln_attn_gain, grad_ln_attn_bias = attn_pull(grad_attn_norm)
    grad_from_mlp, grad_ln_mlp_gain, grad_ln_mlp_bias = mlp_pull(grad_mlp_norm)
    grad_inputs = grad_rows + grad_from_attn + grad_from_mlp
    weight_grads = (
        grad_ln_attn_gain,
        grad_ln_attn_bias,
        grad_ln_mlp_gain,
        grad_ln_mlp_bias,
        grad_qkv_weight,
        grad_content_bias,
        grad_position_bias,
        grad_pos_weight,
        grad_out_weight,
        grad_up_weight,
        grad_up_bias,
        grad_gate_norm_gain,
        grad_gate_norm_bias,
        grad_conv_kernel,
        grad_conv_bias,
        grad_down_weight,
        grad_down_bias,
        grad_merge_weight,
        grad_merge_bias,
    )
    summed = lax.psum(
        (
            weight_grads[0],
            weight_grads[1],
            weight_grads[2],
            weight_grads[3],
            weight_grads[4],
            weight_grads[5],
            weight_grads[6],
            weight_grads[7],
            weight_grads[8],
            weight_grads[9],
            weight_grads[10],
            weight_grads[11],
            weight_grads[12],
            weight_grads[13],
            weight_grads[14],
            weight_grads[15],
            weight_grads[16],
            weight_grads[17],
            weight_grads[18],
        ),
        "tm",
    )
    shares = (
        lax.psum_scatter(
            summed[0].astype(jnp.bfloat16), "stream", scatter_dimension=0, tiled=True
        ).astype(jnp.float32),
        lax.psum_scatter(
            summed[1].astype(jnp.bfloat16), "stream", scatter_dimension=0, tiled=True
        ).astype(jnp.float32),
        lax.psum_scatter(
            summed[2].astype(jnp.bfloat16), "stream", scatter_dimension=0, tiled=True
        ).astype(jnp.float32),
        lax.psum_scatter(
            summed[3].astype(jnp.bfloat16), "stream", scatter_dimension=0, tiled=True
        ).astype(jnp.float32),
        lax.psum_scatter(
            summed[4].astype(jnp.bfloat16), "stream", scatter_dimension=0, tiled=True
        ).astype(jnp.float32),
        lax.psum_scatter(
            summed[5].astype(jnp.bfloat16), "stream", scatter_dimension=0, tiled=True
        ).astype(jnp.float32),
        lax.psum_scatter(
            summed[6].astype(jnp.bfloat16), "stream", scatter_dimension=0, tiled=True
        ).astype(jnp.float32),
        lax.psum_scatter(
            summed[7].astype(jnp.bfloat16), "stream", scatter_dimension=0, tiled=True
        ).astype(jnp.float32),
        lax.psum_scatter(
            summed[8].astype(jnp.bfloat16), "stream", scatter_dimension=0, tiled=True
        ).astype(jnp.float32),
        lax.psum_scatter(
            summed[9].astype(jnp.bfloat16), "stream", scatter_dimension=0, tiled=True
        ).astype(jnp.float32),
        lax.psum_scatter(
            summed[10].astype(jnp.bfloat16), "stream", scatter_dimension=0, tiled=True
        ).astype(jnp.float32),
        lax.psum_scatter(
            summed[11].astype(jnp.bfloat16), "stream", scatter_dimension=0, tiled=True
        ).astype(jnp.float32),
        lax.psum_scatter(
            summed[12].astype(jnp.bfloat16), "stream", scatter_dimension=0, tiled=True
        ).astype(jnp.float32),
        lax.psum_scatter(
            summed[13].astype(jnp.bfloat16), "stream", scatter_dimension=1, tiled=True
        ).astype(jnp.float32),
        lax.psum_scatter(
            summed[14].astype(jnp.bfloat16), "stream", scatter_dimension=0, tiled=True
        ).astype(jnp.float32),
        lax.psum_scatter(
            summed[15].astype(jnp.bfloat16), "stream", scatter_dimension=0, tiled=True
        ).astype(jnp.float32),
        lax.psum_scatter(
            summed[16].astype(jnp.bfloat16), "stream", scatter_dimension=0, tiled=True
        ).astype(jnp.float32),
        lax.psum_scatter(
            summed[17].astype(jnp.bfloat16), "stream", scatter_dimension=0, tiled=True
        ).astype(jnp.float32),
        lax.psum_scatter(
            summed[18].astype(jnp.bfloat16), "stream", scatter_dimension=0, tiled=True
        ).astype(jnp.float32),
    )
    return (out_rows, grad_inputs[None]) + tuple(shares)


LANES = 128
LOW = LANES // 2
BLOCK = 128
TALL = 256
WINDOW = 64
MARGIN = 16
BOUNDS = 16
MEGA = 1024 * 1024
F32 = jnp.float32
BF16 = jnp.bfloat16


def dot_nn(left, right):
    return jnp.dot(left, right, preferred_element_type=F32)


def dot_nt(left, right):
    return lax.dot_general(left, right, (((1,), (1,)), ((), ())), preferred_element_type=F32)


def dot_tn(left, right):
    return lax.dot_general(left, right, (((0,), (0,)), ((), ())), preferred_element_type=F32)


def rows_of(index, size, base=0):
    return pl.ds(pl.multiple_of(index * size, size) + base, size)


def line_of(ref):
    return ref[...].astype(F32).reshape(1, ref.shape[0])


def fold_rows(values):
    return jnp.sum(values.reshape(values.shape[0] // 8, 8, values.shape[1]), axis=0)


def one_row(values):
    return jnp.sum(values, axis=0, keepdims=True)


def turn(values):
    return pltpu.roll(values, LOW, 1)


def low_lanes(rows):
    return lax.broadcasted_iota(jnp.int32, (rows, LANES), 1) < LOW


def centre_rows(inputs):
    mean = jnp.mean(inputs, axis=-1, keepdims=True)
    centred = inputs - mean
    spread = jnp.mean(centred * centred, axis=-1, keepdims=True)
    return centred * lax.rsqrt(spread + EPS)


def gelu_parts(values):
    phi = 0.5 + 0.5 * lax.erf(values * math.sqrt(0.5))
    bell = jnp.exp(values * values * -0.5)
    return values * phi, phi + values * bell * (1.0 / math.sqrt(2.0 * math.pi))


class Part:
    def __init__(self, shape=None, pairs=None, refs=1, late=False):
        self.shape, self.pairs, self.refs, self.late = shape, pairs, refs, late

    def buffer(self, operand):
        return self.shape or operand.shape

    def copies(self, refs, buffer):
        return self.pairs(refs, buffer) if self.pairs else [(refs[0], buffer)]


def blocks_part(half, late=False):
    def pairs(refs, buffer):
        place = lax.axis_index("tm")
        return [
            (
                ref.at[:, pl.ds(half * D, D)],
                buffer.at[rows_of(lax.bitwise_xor(jnp.int32(apart), place), BLOCK)],
            )
            for apart, ref in enumerate(refs)
        ]

    return Part((HEADS * BLOCK, D), pairs, HEADS, late)


def rows_part(first, size, late=False):
    return Part((size, D), lambda refs, buffer: [(refs[0].at[pl.ds(first, size)], buffer)], late=late)


class Fetch:
    def __init__(self, pairs, buffer, sems, first):
        self.buffer, self.begun = buffer, False
        self.pending = [
            pltpu.make_async_copy(source, target, sems.at[first + index])
            for index, (source, target) in enumerate(pairs)
        ]

    def begin(self):
        if not self.begun:
            for copy in self.pending:
                copy.start()
        self.begun = True

    def __call__(self):
        self.begin()
        for copy in self.pending:
            copy.wait()
        self.pending = []
        return self.buffer


def begin(*fetches):
    for fetch in fetches:
        fetch.begin()


class Send:
    def __init__(self, buffer, target, sems):
        self.buffer, self.target, self.sems, self.copies = buffer, target, sems, []

    def go(self, *index):
        source, target = (self.buffer.at[index], self.target.at[index]) if index else (self.buffer, self.target)
        copy = pltpu.make_async_copy(source, target, self.sems[len(self.copies)])
        copy.start()
        self.copies.append(copy)

    def finish(self):
        if not self.copies:
            self.go()


SPACES = {"v": pltpu.VMEM, "s": pltpu.SMEM, "k": pl.ANY}


def kernel_call(body, out_shapes, plan, scratch=(), megas=58, bounds=False, aliases=None):
    def call(*operands):
        in_specs, buffers, at = [], [], 0
        for item in plan:
            if item == "f":
                in_specs.append(pl.BlockSpec(memory_space=pl.ANY))
                buffers.append(pltpu.VMEM(operands[at].shape, operands[at].dtype))
                at += 1
            elif isinstance(item, Part):
                in_specs += [pl.BlockSpec(memory_space=pl.ANY)] * item.refs
                buffers.append(pltpu.VMEM(item.buffer(operands[at]), operands[at].dtype))
                at += item.refs
            else:
                in_specs.append(pl.BlockSpec(memory_space=SPACES[item]))
                at += 1
        sent = [out for out in out_shapes if len(out) > 2]
        buffers += [pltpu.VMEM(out[3] if len(out) > 3 else out[0], out[1]) for out in sent]
        sem_count = 96
        extra = [pltpu.SMEM((BOUNDS,), jnp.int32)] if bounds else []

        def outer(*refs):
            inputs, rest = refs[: len(in_specs)], refs[len(in_specs) :]
            outputs, rest = rest[: len(out_shapes)], rest[len(out_shapes) :]
            held, rest = list(rest[: len(buffers)]), rest[len(buffers) :]
            sems, rest = rest[0], rest[1:]
            given, at, used = [], 0, 0
            for item in plan:
                if item == "f":
                    given.append(Fetch([(inputs[at], held[0])], held.pop(0), sems, used))
                    given[-1].begin()
                    used += 1
                    at += 1
                elif isinstance(item, Part):
                    buffer = held.pop(0)
                    pairs = item.copies(inputs[at : at + item.refs], buffer)
                    given.append(Fetch(pairs, buffer, sems, used))
                    if not item.late:
                        given[-1].begin()
                    used += len(pairs)
                    at += item.refs
                else:
                    given.append(inputs[at])
                    at += 1
            results = []
            for out, ref in zip(out_shapes, outputs):
                if len(out) > 2:
                    target = out[4](ref) if len(out) > 3 else ref
                    results.append(Send(held.pop(0), target, [sems.at[used + index] for index in range(4)]))
                    used += 4
                else:
                    results.append(ref)
            assert used <= sem_count
            given = [item() if kind == "f" else item for kind, item in zip(plan, given)]
            body(*given, *results, *rest)
            for item in given:
                if isinstance(item, Fetch):
                    item()
            sends = [item for item in results if isinstance(item, Send)]
            for item in sends:
                item.finish()
            for item in sends:
                for copy in item.copies:
                    copy.wait()

        return pl.pallas_call(
            outer,
            out_shape=[jax.ShapeDtypeStruct(out[0], out[1]) for out in out_shapes],
            in_specs=in_specs,
            out_specs=[pl.BlockSpec(memory_space=pl.ANY if len(out) > 2 else pltpu.VMEM) for out in out_shapes],
            scratch_shapes=buffers
            + [pltpu.SemaphoreType.DMA((sem_count,))]
            + [pltpu.VMEM(shape, kind) for shape, kind in scratch]
            + extra,
            input_output_aliases=aliases or {},
            compiler_params=pltpu.CompilerParams(vmem_limit_bytes=megas * MEGA),
            cost_estimate=pl.CostEstimate(flops=0, bytes_accessed=0, transcendentals=0),
        )(*operands)

    return call


def fill_bounds(lengths_ref, bounds_s, total):
    bounds_s[0] = jnp.int32(0)
    end = jnp.int32(0)
    for item in range(ITEMS):
        end = end + lengths_ref[0, item]
        bounds_s[item + 1] = end
    for item in range(ITEMS + 1, BOUNDS):
        bounds_s[item] = jnp.int32(total)


def select_kernel(
    up_ref,
    up_bias_ref,
    gain_ref,
    bias_ref,
    conv_bias_ref,
    taps_ref,
    qkv_ref,
    pos_ref,
    content_ref,
    position_ref,
    up_out,
    table_out,
    qkv_out,
    pos_out,
    bias_out,
):
    place = lax.axis_index("tm")
    quarters = lax.axis_size("stream")
    share = HALF // (quarters * lax.axis_size("tm"))
    lane = lax.broadcasted_iota(jnp.int32, (1, 2 * LANES), 1)
    channel = jnp.where(lane < LANES + LOW, lane, lane - LOW)
    group = jnp.zeros_like(channel)
    for quarter in range(1, quarters):
        group = group + (channel >= quarter * share).astype(jnp.int32)
    source = group * (HALF // quarters) + share * place + channel - group * share
    chosen = (lax.broadcasted_iota(jnp.int32, (HALF, 2 * LANES), 0) == source).astype(F32).astype(BF16)
    gate = dot_nn(up_ref[:, :HALF], chosen)
    conv = dot_nn(up_ref[:, HALF:], chosen)
    up_out[:, :LANES] = gate[:, :LANES].astype(BF16)
    up_out[:, LANES : 2 * LANES] = jnp.where(low_lanes(D), gate[:, LANES:], conv[:, LANES:]).astype(BF16)
    up_out[:, 2 * LANES :] = conv[:, :LANES].astype(BF16)
    up_bias = line_of(up_bias_ref)
    lines = jnp.concatenate(
        [
            up_bias[:, :HALF],
            up_bias[:, HALF:],
            line_of(gain_ref),
            line_of(bias_ref),
            line_of(conv_bias_ref),
            jnp.zeros((3, HALF), F32),
        ],
        axis=0,
    )
    lines = dot_nn(lines.astype(BF16), chosen)
    taps = dot_nn(taps_ref[...], chosen)
    for part in range(2):
        lanes = slice(part * LANES, (part + 1) * LANES)
        table_out[part, :8] = lines[:, lanes]
        table_out[part, 8 : 8 + KERNEL] = taps[:, lanes]
        table_out[part, 8 + KERNEL :] = jnp.zeros((1, LANES), F32)

    odd = lax.rem(place, 2) == 1

    def head_lanes(ref, base):
        at = pl.ds(pl.multiple_of(lax.div(place, 2) * LANES + base, LANES), LANES)
        values = ref[:, at].astype(F32)
        values = jnp.where(odd, turn(values), values)
        return jnp.where(low_lanes(values.shape[0]), values, 0.0)

    for part in range(3):
        qkv_out[:, part * LANES : (part + 1) * LANES] = head_lanes(qkv_ref, part * D).astype(BF16)
    pos_out[...] = head_lanes(pos_ref, 0).astype(BF16)
    bias_out[...] = jnp.zeros((8, LANES), F32)
    for line, ref in enumerate((content_ref, position_ref)):
        values = line_of(ref)
        picked = values[:, :LANES]
        for tile in range(1, D // LANES):
            picked = jnp.where(
                lax.div(place, 2) == tile, values[:, tile * LANES : (tile + 1) * LANES], picked
            )
        picked = jnp.where(odd, turn(picked), picked)
        bias_out[line : line + 1] = jnp.where(low_lanes(1), picked, 0.0)


def angle_rows(coarse_ref, fine_ref, block, rows):
    half = D // 2
    base = coarse_ref[pl.ds(block, 1)]
    base_sine, base_cosine = base[:, :half], base[:, half:]
    sine, cosine = fine_ref[rows, :half], fine_ref[rows, half:]
    return base_sine * cosine + base_cosine * sine, base_cosine * cosine - base_sine * sine


def item_codes(bounds_s, index):
    code = jnp.zeros_like(index)
    for item in range(1, ITEMS + 1):
        code = code + (index >= bounds_s[item]).astype(jnp.int32)
    return jnp.where(code < ITEMS, code, ITEMS + index)


def attend_kernel(
    lengths_ref,
    x_ref,
    attn_gain_ref,
    attn_bias_ref,
    mlp_gain_ref,
    mlp_bias_ref,
    qkv_ref,
    pos_ref,
    bias_ref,
    coarse_ref,
    fine_ref,
    up_ref,
    up_bias_ref,
    n_attn_out,
    n_mlp_out,
    hat_out,
    q_position_out,
    query_out,
    key_out,
    value_out,
    prob_out,
    attn_out,
    mean_out,
    rate_out,
    bounds_s,
):
    frames = n_attn_out.buffer.shape[0]
    half = D // 2
    fill_bounds(lengths_ref, bounds_s, frames)
    attn_gain, attn_bias = line_of(attn_gain_ref), line_of(attn_bias_ref)
    mlp_gain, mlp_bias = line_of(mlp_gain_ref), line_of(mlp_bias_ref)
    content, position = bias_ref[0:1], bias_ref[1:2]
    x_ref = x_ref()
    begin(up_ref)

    @pl.loop(0, frames // TALL, unroll=4)
    def _(block):
        rows = rows_of(block, TALL)
        for part in range(TALL // 32):
            at = pl.ds(pl.multiple_of(block * TALL + part * 32, 32), 32)
            hat = centre_rows(x_ref[at].astype(F32))
            hat_out.buffer[at] = hat.astype(BF16)
            n_attn_out.buffer[at] = (hat * attn_gain + attn_bias).astype(BF16)
            n_mlp_out.buffer[at] = (hat * mlp_gain + mlp_bias).astype(BF16)
        parts = dot_nn(n_attn_out.buffer[rows], qkv_ref[...])
        query = parts[:, :LANES]
        query_out.buffer[rows, :LANES] = ((query + content).astype(BF16).astype(F32) * 0.125).astype(BF16)
        q_position = (query + position).astype(BF16)
        q_position_out.buffer[rows] = q_position
        key_out.buffer[rows, :LANES] = parts[:, LANES : 2 * LANES].astype(BF16)
        value_out.buffer[rows] = parts[:, 2 * LANES :].astype(BF16)
        projected = dot_nt(q_position, pos_ref[...])
        for part in range(TALL // 32):
            at = pl.ds(pl.multiple_of(block * TALL + part * 32, 32), 32)
            inner = part * 32 % BLOCK
            sine, cosine = angle_rows(
                coarse_ref, fine_ref, block * (TALL // BLOCK) + part * 32 // BLOCK, slice(inner, inner + 32)
            )
            first = projected[part * 32 : part * 32 + 32, :half]
            second = projected[part * 32 : part * 32 + 32, half:]
            query_out.buffer[at, LANES : LANES + half] = ((first * sine + second * cosine) * 0.125).astype(BF16)
            query_out.buffer[at, LANES + half :] = ((second * sine - first * cosine) * 0.125).astype(BF16)
            key_out.buffer[at, LANES : LANES + half] = cosine.astype(BF16)
            key_out.buffer[at, LANES + half :] = sine.astype(BF16)

    for out in (n_attn_out, n_mlp_out, hat_out, q_position_out, query_out, key_out, value_out):
        out.go()
    up_ref = up_ref()
    up_bias = line_of(up_bias_ref)[:, HALF:]
    @pl.loop(0, frames // TALL, unroll=2)
    def _(block):
        values = dot_nn(n_mlp_out.buffer[rows_of(block, TALL)], up_ref[...])
        for part in range(TALL // 16):
            pre = values[part * 16 : part * 16 + 16] + up_bias
            hidden = pre * (0.5 + 0.5 * lax.erf(pre * math.sqrt(0.5)))
            mean = jnp.mean(hidden, axis=-1, keepdims=True)
            centred = hidden - mean
            rate = lax.rsqrt(jnp.mean(centred * centred, axis=-1, keepdims=True) + EPS)
            at = pl.ds(pl.multiple_of(block * TALL + part * 16, 16), 16)
            mean_out.buffer[at] = jnp.broadcast_to(mean, (16, LANES))
            rate_out.buffer[at] = jnp.broadcast_to(rate, (16, LANES))

    mean_out.go()
    rate_out.go()
    key_code = item_codes(bounds_s, lax.broadcasted_iota(jnp.int32, (1, frames), 1))

    low = low_lanes(32)
    for block in range(frames // TALL):
        rows = pl.ds(block * TALL, TALL)
        raw = dot_nt(query_out.buffer[rows], key_out.buffer[...])
        shares = []
        for part in range(TALL // 32):
            start = block * TALL + part * 32
            index = start + lax.broadcasted_iota(jnp.int32, (32, 1), 0)
            scaled = jnp.where(
                item_codes(bounds_s, index) == key_code, raw[part * 32 : part * 32 + 32], MASKED
            )
            weight = jnp.exp(scaled - jnp.max(scaled, axis=1, keepdims=True))
            prob_out.buffer[pl.ds(start, 32)] = weight.astype(BF16)
            shares.append(1.0 / jnp.sum(weight, axis=1, keepdims=True))
        prob_out.go(rows)
        attn = dot_nn(prob_out.buffer[rows], value_out.buffer[...])
        for part in range(TALL // 32):
            share = shares[part]
            attn_out.buffer[pl.ds(block * TALL + part * 32, 32)] = jnp.where(
                low, attn[part * 32 : part * 32 + 32] * share, share
            )


def fill_margins(wide_s, frames):
    edge = jnp.zeros((MARGIN, LANES), F32)
    wide_s[:MARGIN] = edge
    wide_s[MARGIN + frames : 2 * MARGIN + frames] = edge
    base = frames + 3 * MARGIN
    after = base + frames // 2
    low = low_lanes(MARGIN)
    wide_s[base - MARGIN : base] = jnp.where(low, 0.0, turn(wide_s[after - MARGIN : after]))
    wide_s[after : after + MARGIN] = jnp.where(low, turn(wide_s[base : base + MARGIN]), 0.0)


def item_span(bounds_s, frame):
    begin, end = bounds_s[0], bounds_s[BOUNDS - 1]
    for item in range(1, ITEMS + 1):
        edge = bounds_s[item]
        begin = jnp.where(frame >= edge, edge, begin)
    for item in range(ITEMS, 0, -1):
        edge = bounds_s[item]
        end = jnp.where(frame < edge, edge, end)
    return begin, end


def is_whole(bounds_s, start):
    begin, end = item_span(bounds_s, start)
    reach = KERNEL // 2
    low = (begin == 0) | (begin <= start - reach)
    high = (end == bounds_s[BOUNDS - 1]) | (end >= start + WINDOW + reach)
    return low & high & (end >= start + WINDOW)


def tap_limits(bounds_s, start):
    frame = start + lax.broadcasted_iota(jnp.int32, (WINDOW, LANES), 0)
    begin, end = item_span(bounds_s, frame)
    return begin - frame, end - frame


def grouped(values):
    return values.reshape(WINDOW // 8, 8, LANES)


def triple_places(step, frames):
    half = frames // 2
    return (
        pl.multiple_of(step * WINDOW, 2 * MARGIN),
        pl.multiple_of(step * WINDOW + half, 2 * MARGIN),
        pl.multiple_of(step * WINDOW + frames + 2 * MARGIN, 2 * MARGIN),
    )


def over_windows(bounds_s, frames, body):
    half = frames // 2

    @pl.loop(0, half // WINDOW)
    def _(step):
        start = step * WINDOW
        whole = is_whole(bounds_s, start) & is_whole(bounds_s, start + half)

        @pl.when(whole)
        def _():
            body(step, None)

        @pl.when(jnp.logical_not(whole))
        def _():
            first, second = tap_limits(bounds_s, start), tap_limits(bounds_s, start + half)
            low = low_lanes(WINDOW)
            rest = [jnp.where(low, one, other) for one, other in zip(first, second)]
            body(step, (first, second, rest))


def tap_mask(tap, limits):
    shift = tap - KERNEL // 2
    return None if limits is None else (limits[0] <= shift) & (limits[1] > shift)


def tap_view(window_ref, tap, mask):
    view = window_ref[tap + 1 : tap + 1 + WINDOW]
    return grouped(view if mask is None else jnp.where(mask, view, 0.0))


def mlp_first_kernel(
    lengths_ref,
    n_ref,
    up_ref,
    table_ref,
    mean_ref,
    rate_ref,
    cot_ref,
    merge_ref,
    down_ref,
    attn_ref,
    mixed_out,
    gate_pre_out,
    grad_out,
    rate_out,
    hat_out,
    early_out,
    vectors_out,
    lines_out,
    hat_s,
    slope_s,
    gate_s,
    hidden_s,
    gate_slope_s,
    conv_s,
    grad_s,
    out_s,
    back_s,
    branch_s,
    mix_s,
    taps_s,
    turn_s,
    tap_sum_s,
    columns_s,
    forward_s,
    backward_s,
    bounds_s,
):
    place = lax.axis_index("tm")
    frames = mix_s.shape[0]
    half = frames // 2
    blocks = frames // BLOCK
    quarters, early_rows, _ = early_out.buffer.shape
    share = early_rows // 8
    channels = quarters * share
    fill_bounds(lengths_ref, bounds_s, frames)
    for part in range(2):
        for tap in range(KERNEL):
            line = jnp.broadcast_to(table_ref[part, 8 + tap : 9 + tap], (8, LANES))
            taps_s[part, tap] = line
            turn_s[part, KERNEL - 1 - tap] = line
    tap_sum_s[...] = jnp.zeros(tap_sum_s.shape, F32)
    main, rest = table_ref[0, :8], table_ref[1, :8]
    mixed_bias = jnp.where(low_lanes(1), rest[0:1], rest[1:2])
    low = low_lanes(64)
    gate_pre_ref = gate_pre_out.buffer
    n_ref = n_ref()
    mean_ref, rate_ref = mean_ref(), rate_ref()
    begin(cot_ref, merge_ref, down_ref, attn_ref)

    def stat_rows(rows):
        return mean_ref[rows], rate_ref[rows]

    def chunk(start, base=0):
        return pl.ds(pl.multiple_of(start, 64) + base, 64)

    def conv_part(hidden, mean, rate, lines, rows, to_rows):
        hat = (hidden - mean) * rate
        hat_s[rows] = hat
        hat_out.buffer[rows] = hat.astype(BF16)
        conv_s[to_rows] = (hat * lines[2:3] + lines[3:4]).astype(BF16).astype(F32)

    @pl.loop(0, half // TALL, unroll=2)
    def _(block):
        pre = [dot_nn(n_ref[rows_of(block, TALL, base)], up_ref[...]) for base in (0, half)]
        for part in range(TALL // 64):
            inner = slice(part * 64, part * 64 + 64)
            start = block * TALL + part * 64
            mixed = []
            for values, base in zip(pre, (0, half)):
                rows = chunk(start, base)
                gate, gate_slope = gelu_parts(values[inner, :LANES] + main[0:1])
                hidden_s[rows] = gate
                gate_slope_s[rows] = gate_slope
                hidden, slope = gelu_parts(values[inner, 2 * LANES :] + main[1:2])
                mean, rate = stat_rows(rows)
                slope_s[rows] = slope * rate
                conv_part(hidden, mean, rate, main, rows, chunk(start, base + MARGIN))
                mixed.append((*gelu_parts(values[inner, LANES : 2 * LANES] + mixed_bias), mean, rate))
            (low_hidden, low_slope, low_mean, low_rate), (high_hidden, high_slope, high_mean, high_rate) = mixed
            rows = chunk(start, frames)
            hidden_s[rows] = jnp.where(low, low_hidden, turn(high_hidden))
            gate_slope_s[rows] = jnp.where(low, low_slope, turn(high_slope))
            rate = jnp.where(low, low_rate, high_rate)
            slope_s[rows] = jnp.where(low, turn(low_slope), high_slope) * rate
            conv_part(
                jnp.where(low, turn(low_hidden), high_hidden),
                jnp.where(low, low_mean, high_mean),
                rate,
                rest,
                rows,
                chunk(start, frames + 3 * MARGIN),
            )

    hat_out.go()
    fill_margins(conv_s, frames)
    tall = WINDOW + 2 * MARGIN
    outs = (0, half, frames)

    def convolve(step, limits):
        for index, base in enumerate(triple_places(step, frames)):
            forward_s[index] = conv_s[pl.ds(base, tall)]
        for index in range(3):
            own = None if limits is None else limits[index]
            total = jnp.zeros((WINDOW // 8, 8, LANES), F32)
            for tap in range(KERNEL):
                mask = tap_mask(tap, own)
                total = total + tap_view(forward_s.at[index], tap, mask) * taps_s[index // 2, tap][None]
            lines = rest if index == 2 else main
            out_s[rows_of(step, WINDOW, outs[index])] = total.reshape(WINDOW, LANES) + lines[4:5]

    over_windows(bounds_s, frames, convolve)
    cot_ref = cot_ref()
    merge_ref = merge_ref()
    down_ref = down_ref()
    attn_ref = attn_ref()
    down_ref[channels:] = jnp.zeros((2 * LANES - channels, D), BF16)
    zero = jnp.zeros((8, LANES), F32)

    def branch_part(grad_gated, rows, to_rows, sums):
        up_sum, conv_sum = sums
        gate, conv = hidden_s[rows], out_s[rows]
        gate_pre = (grad_gated * conv * gate_slope_s[rows]).astype(BF16)
        gate_pre_ref[rows] = gate_pre
        grad_conv = (grad_gated * gate).astype(BF16).astype(F32)
        grad_s[to_rows] = grad_conv
        gate_pre = gate_pre.astype(F32)
        return gate * conv, gate_pre, (up_sum + fold_rows(gate_pre), conv_sum + fold_rows(grad_conv))

    def branch_step(block, sums):
        main_sums, rest_sums = sums
        grads = []
        for base in (0, half):
            rows = rows_of(block, TALL, base)
            branch = dot_nt(cot_ref[rows], merge_ref[...]).astype(BF16)
            branch_s[rows] = branch
            grads.append(dot_nt(branch, down_ref[...]))
        for part in range(TALL // 64):
            inner = slice(part * 64, part * 64 + 64)
            start = block * TALL + part * 64
            for values, base in zip(grads, (0, half)):
                rows = chunk(start, base)
                gated, gate_pre, main_sums = branch_part(
                    values[inner, :LANES], rows, chunk(start, base + MARGIN), main_sums
                )
                mix_s[rows, :LANES] = gated.astype(BF16)
                gate_s[rows, :LANES] = gate_pre.astype(BF16)
            grad = jnp.where(low, grads[0][inner, LANES:], turn(grads[1][inner, LANES:]))
            gated, gate_pre, rest_sums = branch_part(
                grad, chunk(start, frames), chunk(start, frames + 3 * MARGIN), rest_sums
            )
            low_rows, high_rows = chunk(start), chunk(start, half)
            gate_s[low_rows, LANES:] = gate_pre.astype(BF16)
            gate_s[high_rows, LANES:] = turn(gate_pre).astype(BF16)
            mix_s[low_rows, LANES:] = jnp.where(low, gated, turn(attn_ref[low_rows])).astype(BF16)
            mix_s[high_rows, LANES:] = jnp.where(low, turn(gated), turn(attn_ref[high_rows])).astype(BF16)
        return main_sums, rest_sums

    (main_up, main_conv), (rest_up, rest_conv) = lax.fori_loop(
        0, half // TALL, branch_step, ((zero, zero), (zero, zero)), unroll=2
    )
    gate_pre_out.go()
    fill_margins(grad_s, frames)
    own = rows_of(place, BLOCK)
    lines_out[0:1] = one_row(fold_rows(branch_s[own].astype(F32)))
    lines_out[1:2] = one_row(fold_rows(cot_ref[own].astype(F32)))
    lines_out[2:8] = jnp.zeros((6, D), F32)
    grad_down = dot_tn(mix_s[...], branch_s[...])
    grad_gate = dot_tn(gate_s[...], n_ref[...])
    for quarter in range(quarters):
        for tile in range(4):
            early_out.buffer[quarter, tile * share : (tile + 1) * share] = grad_down[
                quarter * share : (quarter + 1) * share, tile * LANES : (tile + 1) * LANES
            ].astype(BF16)
        early_out.buffer[quarter, 4 * share :] = grad_gate[
            :channels, quarter * LANES : (quarter + 1) * LANES
        ].astype(BF16)
    early_out.go()
    for block in range(blocks):
        mixed_out.buffer[block, :BLOCK] = mix_s[block * BLOCK : (block + 1) * BLOCK]
    mixed_out.go(slice(None), pl.ds(0, BLOCK))

    def differentiate(step, limits):
        for index, base in enumerate(triple_places(step, frames)):
            forward_s[index] = conv_s[pl.ds(base, tall)]
            backward_s[index] = grad_s[pl.ds(base, tall)]
        for index in range(3):
            own = None if limits is None else limits[index]
            total = jnp.zeros((WINDOW // 8, 8, LANES), F32)
            centre = grouped(backward_s[index, MARGIN : MARGIN + WINDOW])
            for tap in range(KERNEL):
                mask = tap_mask(tap, own)
                total = total + tap_view(backward_s.at[index], tap, mask) * turn_s[index // 2, tap][None]
                tap_sum_s[index // 2, tap] += jnp.sum(tap_view(forward_s.at[index], tap, mask) * centre, axis=0)
            back_s[rows_of(step, WINDOW, outs[index])] = total.reshape(WINDOW, LANES)

    over_windows(bounds_s, frames, differentiate)
    lane = lax.broadcasted_iota(jnp.int32, (64, LANES), 1)

    def norm_part(rows, lines, sums):
        gain_sum, bias_sum = sums
        back, hat, slope = back_s[rows], hat_s[rows], slope_s[rows]
        grad = back * lines[2:3]
        grad_out.buffer[rows] = (grad * slope).astype(BF16)
        rate_out.buffer[rows] = slope.astype(BF16)
        along = back * hat
        return grad, along * lines[2:3], (gain_sum + fold_rows(along), bias_sum + fold_rows(back))

    def norm_step(block, sums):
        main_sums, rest_sums = sums
        for part in range(TALL // 64):
            start = block * TALL + part * 64
            pairs = []
            for base in (0, half):
                plain, along, main_sums = norm_part(chunk(start, base), main, main_sums)
                pairs.append([plain, along])
            plain, along, rest_sums = norm_part(chunk(start, frames), rest, rest_sums)
            for item, values in enumerate((plain, along)):
                pairs[0][item] = pairs[0][item] + jnp.where(low, values, 0.0)
                pairs[1][item] = pairs[1][item] + jnp.where(low, 0.0, values)
            for (plain, along), base in zip(pairs, (0, half)):
                columns_s[chunk(start, base)] = jnp.where(
                    lane == 0,
                    jnp.sum(plain, axis=-1, keepdims=True),
                    jnp.where(lane == 1, jnp.sum(along, axis=-1, keepdims=True), 0.0),
                )
        return main_sums, rest_sums

    (main_gain, main_bias), (rest_gain, rest_bias) = lax.fori_loop(
        0, half // TALL, norm_step, ((zero, zero), (zero, zero)), unroll=2
    )
    grad_out.go()
    rate_out.go()
    totals = jnp.concatenate(
        [jnp.transpose(columns_s[block * BLOCK : (block + 1) * BLOCK])[:2] for block in range(blocks)], axis=0
    )
    high = totals.astype(BF16)
    low_part = (totals - high.astype(F32)).astype(BF16)
    for block in range(blocks):
        mixed_out.buffer[block, BLOCK:, :LANES] = high
        mixed_out.buffer[block, BLOCK:, LANES:] = low_part
    mixed_out.go(slice(None), pl.ds(BLOCK, 2 * blocks))

    def vectors(part, lines):
        taps = jnp.sum(tap_sum_s[part], axis=1)[:KERNEL]
        stacked = jnp.concatenate([taps] + [one_row(line) for line in lines], axis=0)
        if part:
            stacked = stacked + turn(stacked)
        return jnp.transpose(
            jnp.concatenate([stacked, jnp.zeros((LANES - stacked.shape[0], LANES), F32)], axis=0)
        )

    vectors_out[:LANES] = vectors(0, (main_conv, main_gain, main_bias, main_up))
    vectors_out[LANES:] = vectors(1, (rest_conv, rest_gain, rest_bias, rest_up))[: channels - LANES]


def attend_back_kernel(
    cot_ref,
    merge_ref,
    head_ref,
    attn_ref,
    value_ref,
    prob_ref,
    key_ref,
    coarse_ref,
    fine_ref,
    pos_ref,
    query_ref,
    n_ref,
    q_position_ref,
    qkv_ref,
    hat_ref,
    gain_ref,
    early_ref,
    branch_out,
    total_out,
    pack_0,
    pack_1,
    pack_2,
    pack_3,
    lines_out,
    grad_s,
    raw_s,
    projected_s,
    parts_s,
    grads_s,
):
    place = lax.axis_index("tm")
    frames = raw_s.shape[0]
    blocks = frames // BLOCK
    half = D // 2
    zero = jnp.zeros((8, LANES), F32)
    cot_ref, merge_ref, head_ref, attn_ref = cot_ref(), merge_ref(), head_ref(), attn_ref()
    head_ref[HEAD:] = jnp.zeros((LANES - HEAD, D), BF16)
    begin(value_ref, prob_ref, key_ref, pos_ref)

    @pl.loop(0, frames // TALL, unroll=4)
    def _(block):
        rows = rows_of(block, TALL)
        branch = dot_nt(cot_ref[rows], merge_ref[...]).astype(BF16)
        branch_out.buffer[rows] = branch
        grad_s[rows] = (dot_nt(branch, head_ref[...]) * attn_ref[rows, HEAD : HEAD + 1]).astype(BF16)

    branch_out.go()
    value_ref, prob_ref = value_ref(), prob_ref()
    key_ref, pos_ref = key_ref(), pos_ref()
    begin(query_ref, n_ref, q_position_ref, qkv_ref, hat_ref, early_ref)

    def score_step(block, sums):
        content_sum, position_sum = sums
        rows = rows_of(block, TALL)
        grad = grad_s[rows]
        score = dot_nt(grad, value_ref[...])
        for part in range(TALL // 32):
            at = pl.ds(pl.multiple_of(block * TALL + part * 32, 32), 32)
            inner = slice(part * 32, part * 32 + 32)
            delta = jnp.sum(grad[inner].astype(F32) * attn_ref[at], axis=1, keepdims=True)
            raw_s[at] = (prob_ref[at].astype(F32) * (score[inner] - delta)).astype(BF16)
        query = dot_nn(raw_s[rows], key_ref[...]) * 0.125
        for part in range(TALL // 32):
            at = pl.ds(pl.multiple_of(block * TALL + part * 32, 32), 32)
            inner = part * 32 % BLOCK
            sine, cosine = angle_rows(
                coarse_ref, fine_ref, block * (TALL // BLOCK) + part * 32 // BLOCK, slice(inner, inner + 32)
            )
            inner = slice(part * 32, part * 32 + 32)
            first, second = query[inner, LANES : LANES + half], query[inner, LANES + half :]
            projected_s[at, :half] = (first * sine - second * cosine).astype(BF16)
            projected_s[at, half:] = (first * cosine + second * sine).astype(BF16)
        position = dot_nn(projected_s[rows], pos_ref[...])
        content = query[:, :LANES]
        parts_s[rows, :LANES] = (content + position).astype(BF16)
        return content_sum + fold_rows(content), position_sum + fold_rows(position)

    content_sum, position_sum = lax.fori_loop(0, frames // TALL, score_step, (zero, zero), unroll=4)
    query_ref, n_ref, q_position_ref = query_ref(), n_ref(), q_position_ref()
    qkv_ref, hat_ref = qkv_ref(), hat_ref()
    grad_key = dot_tn(query_ref[...], raw_s[...])
    grad_value = dot_tn(grad_s[...], prob_ref[...])
    for block in range(blocks):
        at = slice(block * BLOCK, (block + 1) * BLOCK)
        parts_s[at, LANES : 2 * LANES] = jnp.transpose(grad_key[:, at]).astype(BF16)
        parts_s[at, 2 * LANES :] = jnp.transpose(grad_value[:, at]).astype(BF16)
    grads_s[:HEAD] = dot_tn(parts_s[:, :LANES], n_ref[...])[:HEAD]
    grads_s[HEAD : 2 * HEAD] = dot_nn(grad_key.astype(BF16), n_ref[...])[:HEAD]
    grads_s[2 * HEAD : 3 * HEAD] = dot_nn(grad_value.astype(BF16), n_ref[...])[:HEAD]
    grads_s[3 * HEAD :] = dot_tn(q_position_ref[...], projected_s[...])[:HEAD]
    stream = lax.axis_index("stream")
    early_ref = early_ref()
    for apart, pack_out in enumerate((pack_0, pack_1, pack_2, pack_3)):
        quarter = lax.bitwise_xor(stream, jnp.int32(apart))
        lanes = pl.ds(pl.multiple_of(quarter * LANES, LANES), LANES)
        pack_out.buffer[: 4 * HEAD] = grads_s[:, lanes].astype(BF16)
        pack_out.buffer[4 * HEAD :] = early_ref[quarter]
        pack_out.go()
    gain = line_of(gain_ref)
    wide_zero = jnp.zeros((8, D), F32)

    def norm_step(block, sums):
        gain_sum, bias_sum = sums
        grad = dot_nt(parts_s[rows_of(block, TALL)], qkv_ref[...])
        for part in range(TALL // 32):
            at = pl.ds(pl.multiple_of(block * TALL + part * 32, 32), 32)
            own = grad[part * 32 : part * 32 + 32]
            total_out.buffer[at] = (own * gain).astype(BF16)
            gain_sum = gain_sum + fold_rows(own * hat_ref[at].astype(F32))
            bias_sum = bias_sum + fold_rows(own)
        return gain_sum, bias_sum

    gain_sum, bias_sum = lax.fori_loop(0, frames // TALL, norm_step, (wide_zero, wide_zero), unroll=4)
    lane = lax.broadcasted_iota(jnp.int32, (1, LANES), 1)

    def own_lanes(sums):
        line = one_row(sums)
        line = line + turn(line)
        tiles = [
            jnp.where(lax.div(tile * LANES + lane, HEAD) == place, line, 0.0) for tile in range(D // LANES)
        ]
        return jnp.concatenate(tiles, axis=1)

    lines_out[...] = jnp.concatenate(
        [
            one_row(gain_sum),
            one_row(bias_sum),
            own_lanes(content_sum),
            own_lanes(position_sum),
            jnp.zeros((4, D), F32),
        ],
        axis=0,
    )


def mlp_second_kernel(
    mixed_ref,
    gate_pre_ref,
    grad_ref,
    rate_ref,
    hat_ref,
    up_ref,
    norm_hat_ref,
    gain_ref,
    other_ref,
    pre_out,
    same_out,
    apart_out,
    lines_out,
    up_out,
    columns_s,
):
    place = lax.axis_index("tm")
    pre_s = pre_out.buffer
    frames = pre_s.shape[0]
    half = frames // 2
    blocks = frames // BLOCK
    totals = jnp.zeros((2 * blocks, LANES), F32)
    mixed_ref = mixed_ref()
    for source in range(mixed_ref.shape[0]):
        both = mixed_ref[source].astype(F32)
        totals = totals + (both[:, :LANES] + both[:, LANES:])
    totals = totals * (1.0 / HALF)
    high = totals.astype(BF16)
    low_part = (totals - high.astype(F32)).astype(BF16)
    both = jnp.concatenate([high, low_part], axis=0)
    lane = lax.broadcasted_iota(jnp.int32, (4 * blocks, 2 * LANES), 1) // LANES
    line = lax.broadcasted_iota(jnp.int32, (4 * blocks, 2 * LANES), 0)
    for block in range(blocks):
        chosen = (lax.rem(line, 2 * blocks) == 2 * block + lane).astype(F32).astype(BF16)
        columns_s[block * BLOCK : (block + 1) * BLOCK] = dot_tn(both, chosen)
    gate_pre_ref, grad_ref, rate_ref, hat_ref = gate_pre_ref(), grad_ref(), rate_ref(), hat_ref()
    begin(up_ref, norm_hat_ref, other_ref)
    low = low_lanes(64)
    gain = line_of(gain_ref)

    def chunk(start, base=0):
        return pl.ds(pl.multiple_of(start, 64) + base, 64)

    def pre_part(rows, table, up_sum):
        plain, along = table
        hat, rate = hat_ref[rows].astype(F32), rate_ref[rows].astype(F32)
        pre = (grad_ref[rows].astype(F32) - rate * (plain + hat * along)).astype(BF16).astype(F32)
        return pre, up_sum + fold_rows(pre)

    def pre_step(block, sums):
        main_up, rest_up = sums
        for part in range(TALL // 64):
            start = block * TALL + part * 64
            tables = []
            for base in (0, half):
                rows = chunk(start, base)
                table = [columns_s[rows, item * LANES : (item + 1) * LANES] for item in range(2)]
                tables.append(table)
                pre, main_up = pre_part(rows, table, main_up)
                pre_s[rows, :LANES] = gate_pre_ref[rows]
                pre_s[rows, 2 * LANES :] = pre.astype(BF16)
            rows = chunk(start, frames)
            table = [jnp.where(low, one, other) for one, other in zip(*tables)]
            pre, rest_up = pre_part(rows, table, rest_up)
            gate_pre = gate_pre_ref[rows].astype(F32)
            pre_s[chunk(start), LANES : 2 * LANES] = jnp.where(low, gate_pre, turn(pre)).astype(BF16)
            pre_s[chunk(start, half), LANES : 2 * LANES] = jnp.where(low, turn(gate_pre), pre).astype(BF16)
        return main_up, rest_up

    zero = jnp.zeros((8, LANES), F32)
    main_up, rest_up = lax.fori_loop(0, half // TALL, pre_step, (zero, zero), unroll=2)
    pre_out.go()
    up_ref, norm_hat_ref, other_ref = up_ref(), norm_hat_ref(), other_ref()
    wide_zero = jnp.zeros((8, D), F32)

    def norm_step(step, sums):
        gain_sum, bias_sum = sums
        grads = dot_nt(pre_s[rows_of(step, TALL)], up_ref[...])
        for part in range(TALL // BLOCK):
            block = step * (TALL // BLOCK) + part
            rows = rows_of(block, BLOCK)
            grad = grads[part * BLOCK : (part + 1) * BLOCK]
            total = (grad * gain + other_ref[rows].astype(F32)).astype(BF16)
            apart = lax.bitwise_xor(block, place)

            @pl.when(lax.rem(apart, 2) == 0)
            def _(apart=apart, total=total):
                same_out.buffer[lax.div(apart, 2)] = total

            @pl.when(lax.rem(apart, 2) == 1)
            def _(apart=apart, total=total):
                apart_out.buffer[lax.div(apart, 2)] = total

            gain_sum = gain_sum + fold_rows(grad * norm_hat_ref[rows].astype(F32))
            bias_sum = bias_sum + fold_rows(grad)
        return gain_sum, bias_sum

    gain_sum, bias_sum = lax.fori_loop(0, frames // TALL, norm_step, (wide_zero, wide_zero), unroll=2)
    apart_out.go()
    same_out.go()
    lines_out[...] = jnp.concatenate([one_row(gain_sum), one_row(bias_sum), jnp.zeros((6, D), F32)], axis=0)
    rest_line = one_row(rest_up)
    up_out[:LANES] = jnp.transpose(jnp.broadcast_to(one_row(main_up), (LANES, LANES)))
    up_out[LANES:] = jnp.transpose(jnp.broadcast_to(rest_line + turn(rest_line), (LANES, LANES)))[:LOW]


def late_pack_kernel(
    pre_ref,
    n_ref,
    joined_ref,
    branch_ref,
    cot_ref,
    vectors_ref,
    up_columns_ref,
    first_lines_ref,
    head_lines_ref,
    own_lines_ref,
    pack_out,
):
    pack_ref = pack_out.buffer
    quarters = pack_ref.shape[0]
    channels = vectors_ref.shape[0]
    share = channels // quarters
    gate_at = KERNEL + 3
    lane = lax.broadcasted_iota(jnp.int32, (share, LANES), 1)
    lines = jnp.concatenate(
        [
            head_lines_ref[0:2],
            own_lines_ref[0:2],
            head_lines_ref[2:4],
            first_lines_ref[0:2],
            jnp.zeros((8, D), F32),
        ],
        axis=0,
    )
    for quarter in range(quarters):
        table = vectors_ref[quarter * share : (quarter + 1) * share]
        for other in range(2):
            at = slice((2 * (quarter % 2) + other) * share, (2 * (quarter % 2) + other + 1) * share)
            column = vectors_ref[at, gate_at : gate_at + 1] if quarter < quarters // 2 else up_columns_ref[at, 0:1]
            table = jnp.where(lane == gate_at + other, column, table)
        pack_ref[quarter, channels : channels + share] = table.astype(BF16)
        pack_ref[quarter, channels + share : channels + share + 16] = lines[
            :, quarter * LANES : (quarter + 1) * LANES
        ].astype(BF16)
    grad_up = dot_tn(pre_ref()[...], n_ref()[...])
    for quarter in range(quarters):
        lanes = slice(quarter * LANES, (quarter + 1) * LANES)
        pack_ref[quarter, :LANES] = grad_up[LANES:, lanes].astype(BF16)
        pack_ref[quarter, LANES:channels] = grad_up[LOW:LANES, lanes].astype(BF16)
    joined_ref, cot_ref, branch_ref = joined_ref(), cot_ref(), branch_ref()
    sources, _, rows = joined_ref.shape
    merge_rows = 2 * D // sources
    head_rows = D // sources
    grad_merge = jnp.zeros((merge_rows, D), F32)
    grad_head = jnp.zeros((head_rows, D), F32)
    for source in range(sources):
        at = slice(source * rows, (source + 1) * rows)
        joined = joined_ref[source]
        grad_merge = grad_merge + dot_nn(joined[:merge_rows], cot_ref[at])
        grad_head = grad_head + dot_nn(joined[merge_rows : merge_rows + head_rows], branch_ref[at])
    for quarter in range(quarters):
        base = channels + share + 16
        for grad in (grad_merge, grad_head):
            part = grad.shape[0] // quarters
            for tile in range(4):
                pack_ref[quarter, base : base + part] = grad[
                    quarter * part : (quarter + 1) * part, tile * LANES : (tile + 1) * LANES
                ].astype(BF16)
                base += part


def output_kernel(
    x_ref, mixed_ref, head_ref, down_ref, down_bias_ref, merge_ref, merge_bias_ref, out_ref, joined_out
):
    sources = mixed_ref.shape[0]
    rows = x_ref.shape[0]
    channels = HALF // sources
    share = channels // 4
    attn_parts = []
    branch_attn = jnp.zeros((rows, D), F32)
    branch_mlp = jnp.zeros((rows, D), F32)
    for source in range(sources):
        attn = turn(mixed_ref[source, :rows, LANES:].astype(F32))[:, :HEAD].astype(BF16)
        attn_parts.append(attn)
        branch_attn = branch_attn + dot_nn(attn, head_ref[source * HEAD : (source + 1) * HEAD])
        down = jnp.concatenate(
            [down_ref[(part * sources + source) * share : (part * sources + source + 1) * share] for part in range(4)],
            axis=0,
        )
        branch_mlp = branch_mlp + dot_nn(mixed_ref[source, :rows, :channels], down)
    joined = jnp.concatenate(
        [branch_attn.astype(BF16), (branch_mlp + line_of(down_bias_ref)).astype(BF16)], axis=1
    )
    result = x_ref[...].astype(F32) + dot_nn(joined, merge_ref[...]) + line_of(merge_bias_ref)
    out_ref[...] = result.astype(BF16)
    turned = jnp.transpose(joined.astype(F32))
    heads = jnp.transpose(jnp.concatenate(attn_parts, axis=1).astype(F32))
    merge_share = turned.shape[0] // (4 * sources)
    head_share = heads.shape[0] // (4 * sources)
    used = 4 * (merge_share + head_share)
    for target in range(sources):
        for part in range(4):
            at = (part * sources + target) * merge_share
            joined_out[target, part * merge_share : (part + 1) * merge_share] = turned[
                at : at + merge_share
            ].astype(BF16)
            at = (part * sources + target) * head_share
            to = 4 * merge_share + part * head_share
            joined_out[target, to : to + head_share] = heads[at : at + head_share].astype(BF16)
        joined_out[target, used:] = jnp.zeros((joined_out.shape[1] - used, rows), BF16)


def pair_kernel(same_ref, other_ref, *out_refs):
    for slot, out_ref in enumerate(out_refs):
        out_ref[...] = (same_ref[slot].astype(F32) + other_ref[slot].astype(F32)).astype(BF16)


def frames_kernel(x_ref, cot_ref, *refs):
    total_refs, out_ref = refs[:-1], refs[-1]
    for part in range(x_ref.shape[0] // 32):
        rows = slice(part * 32, part * 32 + 32)
        inputs = x_ref[rows].astype(F32)
        mean = jnp.mean(inputs, axis=-1, keepdims=True)
        centred = inputs - mean
        rate = lax.rsqrt(jnp.mean(centred * centred, axis=-1, keepdims=True) + EPS)
        hat = centred * rate
        grad = total_refs[0][rows].astype(F32)
        for total_ref in total_refs[1:]:
            grad = grad + total_ref[rows].astype(F32)
        plain = jnp.mean(grad, axis=-1, keepdims=True)
        along = jnp.mean(grad * hat, axis=-1, keepdims=True)
        out_ref[rows] = cot_ref[rows].astype(F32) + rate * (grad - plain - hat * along)


def add_kernel(*refs):
    out_ref = refs[-1]
    first = 0
    for at in range(0, len(refs) - 1, 4):
        total = refs[at][...].astype(F32)
        for ref in refs[at + 1 : at + 4]:
            total = total + ref[...].astype(F32)
        out_ref[first : first + total.shape[0]] = total.astype(BF16)
        first += total.shape[0]


def gather_parts(near_ref, far_ref, all_s):
    place = lax.axis_index("tm")
    for apart in range(all_s.shape[0]):
        part_ref = far_ref if apart % 2 else near_ref
        all_s[lax.bitwise_xor(jnp.int32(apart), place)] = part_ref[apart // 2]


def lines_from(all_s, base, size):
    return jnp.concatenate([all_s[source, base : base + size] for source in range(all_s.shape[0])], axis=0).astype(F32)


def add_streams_kernel(parts_ref, out_ref):
    total = parts_ref[0].astype(F32)
    for source in range(1, parts_ref.shape[0]):
        total = total + parts_ref[source].astype(F32)
    out_ref[...] = total.astype(BF16)


def early_kernel(near_ref, far_ref, qkv_out, pos_out, down_out, up_out, all_s):
    gather_parts(near_ref, far_ref, all_s)
    sources = all_s.shape[0]
    share = HALF // (4 * sources)
    for kind in range(4):
        lines = jnp.transpose(lines_from(all_s, kind * HEAD, HEAD))
        if kind < 3:
            qkv_out[:, kind * D : (kind + 1) * D] = lines
        else:
            pos_out[...] = lines
    base = 4 * HEAD
    for source in range(sources):
        for tile in range(4):
            down_out[source * share : (source + 1) * share, tile * LANES : (tile + 1) * LANES] = all_s[
                source, base + tile * share : base + (tile + 1) * share
            ].astype(F32)
    wide = sources * share
    for group in range(4):
        up_out.buffer[:, group * wide : (group + 1) * wide] = jnp.transpose(
            lines_from(all_s, base + 4 * share + group * share, share)
        )


def late_kernel(*refs):
    _, near_ref, far_ref = refs[:3]
    (
        attn_gain_out,
        attn_bias_out,
        mlp_gain_out,
        mlp_bias_out,
        content_out,
        position_out,
        outw_out,
        up_out,
        up_bias_out,
        gain_out,
        bias_out,
        taps_out,
        conv_bias_out,
        down_bias_out,
        merge_out,
        merge_bias_out,
        all_s,
    ) = refs[3:]
    gather_parts(near_ref, far_ref, all_s)
    sources = all_s.shape[0]
    channels = HALF // sources
    share = channels // 4
    merge_share = 2 * D // (4 * sources)
    head_share = D // (4 * sources)
    base = channels + share + 16
    for source in range(sources):
        for tile in range(4):
            lanes = slice(tile * LANES, (tile + 1) * LANES)
            at = base + tile * merge_share
            merge_out.buffer[source * merge_share : (source + 1) * merge_share, lanes] = all_s[
                source, at : at + merge_share
            ].astype(F32)
            at = base + 4 * merge_share + tile * head_share
            outw_out.buffer[source * head_share : (source + 1) * head_share, lanes] = all_s[
                source, at : at + head_share
            ].astype(F32)
    merge_out.go()
    outw_out.go()
    base = 0
    for group in range(4):
        at = group * sources * share
        up_out.buffer[:, at : at + sources * share] = jnp.transpose(lines_from(all_s, base + group * share, share))
    up_out.go()
    table = jnp.transpose(lines_from(all_s, base + channels, share))
    taps_out[...] = table[:KERNEL]
    conv_bias_out[...] = table[KERNEL]
    gain_out[...] = table[KERNEL + 1]
    bias_out[...] = table[KERNEL + 2]
    wide = sources * share
    up_bias_out[:wide] = table[KERNEL + 3]
    up_bias_out[wide:] = table[KERNEL + 4]
    base = base + channels + share
    lines = all_s[0, base : base + 16].astype(F32)
    for source in range(1, sources):
        lines = lines + all_s[source, base : base + 16].astype(F32)
    outs = (attn_gain_out, attn_bias_out, mlp_gain_out, mlp_bias_out, content_out, position_out, down_bias_out, merge_bias_out)
    for line, out in enumerate(outs):
        out[...] = lines[line]


def moved(block, axis, bits):
    count = lax.axis_size(axis)
    return lax.ppermute(block, axis, [(index, index ^ bits) for index in range(count)])


def over_streams(packs):
    return [packs[0]] + [moved(packs[bits], "stream", bits) for bits in range(1, lax.axis_size("stream"))]


def near_blocks(block):
    return [block] + [moved(block, "tm", bits) for bits in range(2, lax.axis_size("tm"), 2)]


def far_blocks(near):
    far = [moved(part, "tm", 1) for part in near]
    return [part for pair in zip(near, far) for part in pair]


def far_stack(near):
    stack = jnp.stack(near)
    return stack, moved(stack, "tm", 1)


def head_device(
    frames,
    lengths,
    cotangent,
    ln_attn_gain,
    ln_attn_bias,
    ln_mlp_gain,
    ln_mlp_bias,
    qkv_weight,
    content_bias,
    position_bias,
    pos_weight,
    out_weight,
    up_weight,
    up_bias,
    gate_norm_gain,
    gate_norm_bias,
    conv_kernel,
    conv_bias,
    down_weight,
    down_bias,
    merge_weight,
    merge_bias,
):
    count = lax.axis_size("tm")
    quarters = lax.axis_size("stream")
    own = frames.shape[1]
    total = own * count
    folded = total + total // 2
    padded = folded + 4 * MARGIN
    share = HALF // (quarters * count)
    channels = HALF // count
    quarter = D // quarters
    own_frames = frames[0]
    own_cotangent = cotangent[0]

    whole, late = Part(), Part(late=True)
    near = near_blocks(jnp.concatenate([own_frames, own_cotangent], axis=1))
    up_own, table, qkv_own, pos_own, bias_own = kernel_call(
        select_kernel,
        [
            ((D, 3 * LANES), BF16),
            ((2, 8 + KERNEL + 1, LANES), F32),
            ((D, 3 * LANES), BF16),
            ((D, LANES), BF16),
            ((8, LANES), F32),
        ],
        10 * "v",
    )(
        up_weight,
        up_bias,
        gate_norm_gain,
        gate_norm_bias,
        conv_bias,
        conv_kernel,
        qkv_weight,
        pos_weight,
        content_bias,
        position_bias,
    )
    frequency = jnp.exp(jnp.arange(D // 2, dtype=F32) * (-2.0 * math.log(10000.0) / D))
    coarse = jnp.arange(0, total, BLOCK, dtype=F32)[:, None] * frequency[None]
    fine = jnp.arange(BLOCK, dtype=F32)[:, None] * frequency[None]
    coarse_table = jnp.concatenate([jnp.sin(coarse), jnp.cos(coarse)], axis=1)
    fine_table = jnp.concatenate([jnp.sin(fine), jnp.cos(fine)], axis=1)
    near, up_own, coarse_table, fine_table = lax.optimization_barrier((near, up_own, coarse_table, fine_table))
    blocks = far_blocks(near)

    n_attn, n_mlp, hat, q_position, query, key, value, prob, attn, mean, rate = kernel_call(
        attend_kernel,
        [
            ((total, D), BF16, 1),
            ((total, D), BF16, 1),
            ((total, D), BF16, 1),
            ((total, LANES), BF16, 1),
            ((total, LANES + D), BF16, 1),
            ((total, LANES + D), BF16, 1),
            ((total, LANES), BF16, 1),
            ((total, total), BF16, 1),
            ((total, LANES), F32, 1),
            ((total, LANES), F32, 1),
            ((total, LANES), F32, 1),
        ],
        [
            "s",
            blocks_part(0),
            *"vvvvvvvvv",
            Part((D, HALF), lambda refs, buffer: [(refs[0].at[:, pl.ds(HALF, HALF)], buffer)], late=True),
            "v",
        ],
        bounds=True,
    )(
        lengths,
        *blocks,
        ln_attn_gain,
        ln_attn_bias,
        ln_mlp_gain,
        ln_mlp_bias,
        qkv_own,
        pos_own,
        bias_own,
        coarse_table,
        fine_table,
        up_weight,
        up_bias,
    )

    def own_down(refs, buffer):
        place = lax.axis_index("tm")
        stride = HALF // quarters
        return [
            (
                refs[0].at[pl.ds(pl.multiple_of(part * stride + share * place, 16), share)],
                buffer.at[pl.ds(part * share, share)],
            )
            for part in range(quarters)
        ]

    mixed, gate_pre, grad_y, slope, gate_hat, early_pack, vectors, first_lines = kernel_call(
        mlp_first_kernel,
        [
            ((count, own + 16, 2 * LANES), BF16, 1),
            ((folded, LANES), BF16, 1),
            ((folded, LANES), BF16, 1),
            ((folded, LANES), BF16, 1),
            ((folded, LANES), BF16, 1),
            ((quarters, 8 * share, LANES), BF16, 1),
            ((channels, LANES), F32),
            ((8, D), F32),
        ],
        [
            "s",
            whole,
            "v",
            "v",
            whole,
            whole,
            blocks_part(1, late=True),
            rows_part(D, D, late=True),
            Part((2 * LANES, D), own_down, late=True),
            Part(late=True),
        ],
        [
            ((folded, LANES), F32),
            ((folded, LANES), F32),
            ((total, 2 * LANES), BF16),
            ((folded, LANES), F32),
            ((folded, LANES), F32),
            ((padded, LANES), F32),
            ((padded, LANES), F32),
            ((folded, LANES), F32),
            ((folded, LANES), F32),
            ((total, D), BF16),
            ((total, 2 * LANES), BF16),
            ((2, 32, 8, LANES), F32),
            ((2, 32, 8, LANES), F32),
            ((2, 32, 8, LANES), F32),
            ((total, LANES), F32),
            ((3, WINDOW + 2 * MARGIN, LANES), F32),
            ((3, WINDOW + 2 * MARGIN, LANES), F32),
        ],
        bounds=True,
    )(lengths, n_mlp, up_own, table, mean, rate, *blocks, merge_weight, down_weight, attn)
    mixed_own = lax.all_to_all(mixed, "tm", 0, 0, tiled=True)

    def own_head(refs, buffer):
        at = pl.ds(pl.multiple_of(lax.axis_index("tm") * HEAD, HEAD), HEAD)
        return [(refs[0].at[at], buffer.at[pl.ds(0, HEAD)])]

    branch, from_attn, *head_packs, head_lines = kernel_call(
        attend_back_kernel,
        [
            ((total, D), BF16, 1),
            ((total, D), BF16, 1),
            *([((4 * HEAD + 8 * share, LANES), BF16, 1)] * quarters),
            ((8, D), F32),
        ],
        [
            blocks_part(1),
            rows_part(0, D),
            Part((LANES, D), own_head),
            whole,
            late,
            late,
            late,
            "v",
            "v",
            late,
            Part((total, LANES), lambda refs, buffer: [(refs[0].at[:, pl.ds(0, LANES)], buffer)], late=True),
            late,
            late,
            late,
            late,
            "v",
            late,
        ],
        [
            ((total, LANES), BF16),
            ((total, total), BF16),
            ((total, D), BF16),
            ((total, 3 * LANES), BF16),
            ((4 * HEAD, D), F32),
        ],
    )(
        *blocks,
        merge_weight,
        out_weight,
        attn,
        value,
        prob,
        key,
        coarse_table,
        fine_table,
        pos_own,
        query,
        n_attn,
        q_position,
        qkv_own,
        hat,
        ln_attn_gain,
        early_pack,
    )
    head_parts = over_streams(head_packs)
    mixed_own, _ = lax.optimization_barrier((mixed_own, head_lines))
    out_rows, joined = kernel_call(
        output_kernel,
        [((own, D), BF16), ((count, 256, own), BF16)],
        "vvvvvvv",
        megas=24,
    )(own_frames, mixed_own, out_weight, down_weight, down_bias, merge_weight, merge_bias)
    joined_all = lax.all_to_all(joined, "tm", 0, 0, tiled=True)
    gate_pre, _ = lax.optimization_barrier((gate_pre, joined))
    late_rows = 5 * share + 16 + 3 * D // count
    pre, same, apart, own_lines, up_columns = kernel_call(
        mlp_second_kernel,
        [
            ((total, 3 * LANES), BF16, 1),
            ((count // 2, own, D), BF16, 1),
            ((count // 2, own, D), BF16, 1),
            ((8, D), F32),
            ((channels, LANES), F32),
        ],
        [
            Part(
                (count, 2 * total // BLOCK, 2 * LANES),
                lambda refs, buffer: [(refs[0].at[:, pl.ds(own, 2 * total // BLOCK)], buffer)],
            ),
            *([whole] * 4),
            late,
            late,
            "v",
            late,
        ],
        [((total, 2 * LANES), F32)],
    )(mixed_own, gate_pre, grad_y, slope, gate_hat, up_own, hat, ln_mlp_gain, from_attn)
    pre, head_parts = lax.optimization_barrier((pre, head_parts))
    (early_part,) = kernel_call(add_kernel, [((4 * HEAD + 8 * share, LANES), BF16)], quarters * "v", megas=24)(
        *head_parts
    )
    pre, joined_all, early_part = lax.optimization_barrier((pre, joined_all, early_part))
    early_near = near_blocks(early_part)
    (late_pack,) = kernel_call(
        late_pack_kernel,
        [((quarters, late_rows, LANES), BF16, 1)],
        [
            Part(
                (total, 2 * LANES),
                lambda refs, buffer: [(refs[0].at[:, pl.ds(LANES, 2 * LANES)], buffer)],
            ),
            whole,
            whole,
            whole,
            blocks_part(1),
            *"vvvvv",
        ],
    )(pre, n_mlp, joined_all, branch, *blocks, vectors, up_columns, first_lines, head_lines, own_lines)
    late_pack, early_near = lax.optimization_barrier((late_pack, early_near))
    late_moved = lax.all_to_all(late_pack, "stream", 0, 0, tiled=True)
    apart, _ = lax.optimization_barrier((apart, late_pack))
    sibling = moved(apart, "tm", 1)
    pairs = kernel_call(pair_kernel, [((own, D), BF16)] * (count // 2), "vv", megas=24)(same, sibling)
    sums = [pairs[0]] + [moved(pairs[slot], "tm", 2 * slot) for slot in range(1, count // 2)]
    early_all = far_stack(early_near)
    grad_qkv, grad_pos, grad_down, half_up = kernel_call(
        early_kernel,
        [
            ((quarter, 3 * D), F32),
            ((quarter, D), F32),
            ((HALF // quarters, D), F32),
            ((quarter, 2 * HALF), F32, 1, (quarter, HALF), lambda ref: ref.at[:, pl.ds(0, HALF)]),
        ],
        "vv",
        [((count, 4 * HEAD + 8 * share, LANES), BF16)],
        megas=24,
    )(*early_all)
    late_moved, grad_pos, sums = lax.optimization_barrier((late_moved, grad_pos, sums))
    (late_part,) = kernel_call(add_streams_kernel, [((late_rows, LANES), BF16)], "v", megas=24)(late_moved)
    late_near = near_blocks(late_part)
    (grad_frames,) = kernel_call(frames_kernel, [((own, D), F32)], (2 + count // 2) * "v", megas=24)(
        own_frames, own_cotangent, *sums
    )
    late_near, grad_frames = lax.optimization_barrier((late_near, grad_frames))
    late_parts = far_stack(late_near)
    late = kernel_call(
        late_kernel,
        [((quarter,), F32)] * 6
        + [
            ((quarter, D), F32, 1),
            ((quarter, 2 * HALF), F32, 1, (quarter, HALF), lambda ref: ref.at[:, pl.ds(HALF, HALF)]),
            ((2 * HALF // quarters,), F32),
            ((HALF // quarters,), F32),
            ((HALF // quarters,), F32),
            ((KERNEL, HALF // quarters), F32),
            ((HALF // quarters,), F32),
            ((quarter,), F32),
            ((2 * D // quarters, D), F32, 1),
            ((quarter,), F32),
        ],
        "kvv",
        [((count,) + late_part.shape, BF16)],
        megas=24,
        aliases={0: 7},
    )(half_up, *late_parts)
    return (
        out_rows[None],
        grad_frames[None],
        *late[:4],
        grad_qkv,
        *late[4:6],
        grad_pos,
        *late[6:13],
        grad_down,
        *late[13:],
    )


def per_device(*operands):
    fits = (
        lax.axis_size("tm") == HEADS
        and lax.axis_size("stream") * LANES == D
        and operands[0].shape[1] == BLOCK
    )
    return head_device(*operands) if fits else frame_device(*operands)


def solution(mesh):
    return jax.shard_map(
        per_device,
        mesh=mesh,
        in_specs=(
            P("stream", "tm", None),
            P("stream", None),
            P("stream", "tm", None),
            P(),
            P(),
            P(),
            P(),
            P(),
            P(),
            P(),
            P(),
            P(),
            P(),
            P(),
            P(),
            P(),
            P(),
            P(),
            P(),
            P(),
            P(),
            P(),
        ),
        out_specs=(
            P("stream", "tm", None),
            P("stream", "tm", None),
            P("stream"),
            P("stream"),
            P("stream"),
            P("stream"),
            P("stream", None),
            P("stream"),
            P("stream"),
            P("stream", None),
            P("stream", None),
            P("stream", None),
            P("stream"),
            P("stream"),
            P("stream"),
            P(None, "stream"),
            P("stream"),
            P("stream", None),
            P("stream"),
            P("stream", None),
            P("stream"),
        ),
        check_vma=False,
    )
```

```python
import math

import jax
import jax.numpy as jnp
from jax import lax
from jax.experimental import pallas as pl
from jax.experimental.pallas import tpu as pltpu
from jax.sharding import PartitionSpec as P

D = 512
HEADS = 8
HEAD = 64
KERNEL = 31
ITEMS = 5
HALF = 1536


EPS = 1e-05
MASKED = -1e30


def extended(block, sides, width):
    for axis, dim in sides:
        count = lax.axis_size(axis)
        forward = [(i, i + 1) for i in range(count - 1)]
        backward = [(target, source) for source, target in forward]
        low = lax.ppermute(
            lax.slice_in_dim(block, block.shape[dim] - width, None, axis=dim), axis, forward
        )
        high = lax.ppermute(lax.slice_in_dim(block, 0, width, axis=dim), axis, backward)
        block = jnp.concatenate([low, block, high], axis=dim)
    return block


def norm_rows(inputs, scale_row, shift_row):
    row_mean = jnp.mean(inputs, axis=-1, keepdims=True)
    centred = inputs - row_mean
    spread = jnp.mean(centred * centred, axis=-1, keepdims=True)
    return centred * lax.rsqrt(spread + EPS) * scale_row + shift_row


def gelu_exact(inputs):
    return jax.nn.gelu(inputs, approximate=False)


def frame_info(lengths, offset, extent):
    item_ends = jnp.cumsum(lengths)
    first_table = jnp.concatenate([item_ends - lengths, item_ends[-1:]])
    frame_index = offset + jnp.arange(extent, dtype=jnp.int32)
    item_of = jnp.sum((frame_index[:, None] >= item_ends[None, :]).astype(jnp.int32), axis=1)
    labels = jnp.arange(ITEMS + 1, dtype=jnp.int32)
    first_frame = jnp.sum(
        jnp.where(item_of[:, None] == labels[None, :], first_table[None, :], 0), axis=1
    )
    return (frame_index, item_of, frame_index - first_frame)


def angles(place_in):
    frequency = jnp.exp(jnp.arange(D // 2, dtype=jnp.float32) * (-2.0 * math.log(10000.0) / D))
    phase_angle = place_in.astype(jnp.float32)[:, None] * frequency[None, :]
    return (jnp.sin(phase_angle), jnp.cos(phase_angle))


def rel_query(projected, sine_rows, cosine_rows):
    half_size = projected.shape[-1] // 2
    first_half = projected[..., :half_size]
    second_half = projected[..., half_size:]
    sine_wide = sine_rows[:, None, :]
    cosine_wide = cosine_rows[:, None, :]
    return jnp.concatenate(
        [
            first_half * sine_wide + second_half * cosine_wide,
            second_half * sine_wide - first_half * cosine_wide,
        ],
        axis=-1,
    )


def step_size(extent):
    return math.gcd(extent, 512)


def score_block(q_content, q_rel, query_item, query_frame, key_block, key_start, lengths):
    extent = key_block.shape[0]
    key_frame, key_item, key_place = frame_info(lengths, key_start, extent)
    sine_rows, cosine_rows = angles(key_place)
    k_rel = jnp.concatenate([cosine_rows, sine_rows], axis=1).astype(jnp.bfloat16)
    raw_scores = jnp.einsum(
        "qhe,khe->hqk",
        q_content,
        key_block.reshape(extent, HEADS, HEAD),
        preferred_element_type=jnp.float32,
    )
    raw_scores = raw_scores + jnp.einsum(
        "qhc,kc->hqk", q_rel, k_rel, preferred_element_type=jnp.float32
    )
    allowed = (query_item[:, None] == key_item[None, :]) & (
        (query_item[:, None] < ITEMS) | (query_frame[:, None] == key_frame[None, :])
    )
    return (raw_scores, allowed, k_rel)


def block_grads(
    q_content,
    q_rel,
    query_item,
    query_frame,
    grad_out,
    log_total,
    delta_rows,
    key_block,
    value_block,
    key_start,
    lengths,
):
    extent = key_block.shape[0]
    raw_scores, allowed, k_rel = score_block(
        q_content, q_rel, query_item, query_frame, key_block, key_start, lengths
    )
    prob_rows = jnp.where(allowed[None], jnp.exp(raw_scores * 0.125 - log_total[:, :, None]), 0.0)
    grad_prob = jnp.einsum(
        "qhe,khe->hqk",
        grad_out,
        value_block.reshape(extent, HEADS, HEAD),
        preferred_element_type=jnp.float32,
    )
    grad_raw = (prob_rows * (grad_prob - delta_rows[:, :, None]) * 0.125).astype(jnp.bfloat16)
    return (prob_rows.astype(jnp.bfloat16), grad_raw, k_rel)


def frame_device(
    frames,
    lengths,
    cotangent,
    ln_attn_gain,
    ln_attn_bias,
    ln_mlp_gain,
    ln_mlp_bias,
    qkv_weight,
    content_bias,
    position_bias,
    pos_weight,
    out_weight,
    up_weight,
    up_bias,
    gate_norm_gain,
    gate_norm_bias,
    conv_kernel,
    conv_bias,
    down_weight,
    down_bias,
    merge_weight,
    merge_bias,
):
    row_count = frames.shape[1]
    cycle_size = lax.axis_size("tm")
    offset = lax.axis_index("tm") * row_count
    stream_lengths = lengths[0]
    inputs = frames[0].astype(jnp.float32)
    frame_index, item_of, place_in = frame_info(stream_lengths, offset, row_count)
    sine_rows, cosine_rows = angles(place_in)
    attn_norm, attn_pull = jax.vjp(
        norm_rows, inputs, ln_attn_gain.astype(jnp.float32), ln_attn_bias.astype(jnp.float32)
    )
    mlp_norm, mlp_pull = jax.vjp(
        norm_rows, inputs, ln_mlp_gain.astype(jnp.float32), ln_mlp_bias.astype(jnp.float32)
    )
    attn_norm_low = attn_norm.astype(jnp.bfloat16)
    mlp_norm_low = mlp_norm.astype(jnp.bfloat16)
    qkv_rows = jnp.dot(attn_norm_low, qkv_weight, preferred_element_type=jnp.float32)
    query_rows = qkv_rows[:, :D]
    key_rows = qkv_rows[:, D : 2 * D].astype(jnp.bfloat16)
    value_rows = qkv_rows[:, 2 * D :].astype(jnp.bfloat16)
    q_content = (query_rows + content_bias.astype(jnp.float32)).astype(jnp.bfloat16)
    q_position = (query_rows + position_bias.astype(jnp.float32)).astype(jnp.bfloat16)
    content_heads = q_content.reshape(row_count, HEADS, HEAD)
    position_heads = q_position.reshape(row_count, HEADS, HEAD)
    pos_heads = pos_weight.reshape(D, HEADS, HEAD)
    projected = jnp.einsum(
        "the,che->thc", position_heads, pos_heads, preferred_element_type=jnp.float32
    )
    q_rel = rel_query(projected, sine_rows, cosine_rows).astype(jnp.bfloat16)
    start_state = (
        jnp.full((HEADS, row_count), MASKED, jnp.float32),
        jnp.zeros((HEADS, row_count), jnp.float32),
        jnp.zeros((HEADS, row_count, HEAD), jnp.float32),
    )
    fold_state = start_state
    key_piece = lax.all_gather(key_rows, "tm", axis=0, tiled=True)
    value_piece = lax.all_gather(value_rows, "tm", axis=0, tiled=True)
    extent = key_piece.shape[0]
    step_rows = step_size(extent)

    def forward_one_step(inner_state, step_index):
        row_top, row_total, row_acc = inner_state
        key_block = lax.dynamic_slice_in_dim(key_piece, step_index * step_rows, step_rows, 0)
        value_block = lax.dynamic_slice_in_dim(value_piece, step_index * step_rows, step_rows, 0)
        raw_scores, allowed, k_rel = score_block(
            content_heads,
            q_rel,
            item_of,
            frame_index,
            key_block,
            step_index * step_rows,
            stream_lengths,
        )
        scaled = jnp.where(allowed[None], raw_scores * 0.125, MASKED)
        new_top = jnp.maximum(row_top, jnp.max(scaled, axis=2))
        weight = jnp.where(allowed[None], jnp.exp(scaled - new_top[:, :, None]), 0.0)
        factor = jnp.exp(row_top - new_top)
        row_total = row_total * factor + jnp.sum(weight, axis=2)
        row_acc = row_acc * factor[:, :, None] + jnp.einsum(
            "hqk,khe->hqe",
            weight.astype(jnp.bfloat16),
            value_block.reshape(step_rows, HEADS, HEAD),
            preferred_element_type=jnp.float32,
        )
        return ((new_top, row_total, row_acc), None)

    fold_state, unused = lax.scan(
        forward_one_step, fold_state, jnp.arange(extent // step_rows, dtype=jnp.int32)
    )
    row_top, row_total, row_acc = fold_state
    attn_heads = row_acc / row_total[:, :, None]
    log_total = row_top + jnp.log(row_total)
    attn_low = jnp.transpose(attn_heads, (1, 0, 2)).reshape(row_count, D).astype(jnp.bfloat16)
    branch_attn = jnp.dot(attn_low, out_weight, preferred_element_type=jnp.float32).astype(
        jnp.bfloat16
    )
    hidden_pre = jnp.dot(
        mlp_norm_low, up_weight, preferred_element_type=jnp.float32
    ) + up_bias.astype(jnp.float32)
    hidden, gelu_pull = jax.vjp(gelu_exact, hidden_pre)
    gate_half = hidden[:, :HALF]
    conv_norm, conv_pull = jax.vjp(
        norm_rows,
        hidden[:, HALF:],
        gate_norm_gain.astype(jnp.float32),
        gate_norm_bias.astype(jnp.float32),
    )
    conv_in = conv_norm.astype(jnp.bfloat16)
    half_width = KERNEL // 2
    conv_wide = extended(conv_in, (("tm", 0),), half_width)
    wide_frame, wide_item, wide_place = frame_info(
        stream_lengths, offset - half_width, row_count + 2 * half_width
    )
    kernel_rows = conv_kernel.astype(jnp.float32)
    conv_out = conv_bias.astype(jnp.float32) + jnp.zeros_like(gate_half)
    for tap_index in range(KERNEL):
        same_item = (wide_item[tap_index : tap_index + row_count] == item_of)[:, None]
        conv_out = (
            conv_out
            + jnp.where(
                same_item, conv_wide[tap_index : tap_index + row_count].astype(jnp.float32), 0.0
            )
            * kernel_rows[tap_index]
        )
    gated_low = (gate_half * conv_out).astype(jnp.bfloat16)
    branch_mlp = (
        jnp.dot(gated_low, down_weight, preferred_element_type=jnp.float32)
        + down_bias.astype(jnp.float32)
    ).astype(jnp.bfloat16)
    joined = jnp.concatenate([branch_attn, branch_mlp], axis=1)
    result = (
        inputs
        + jnp.dot(joined, merge_weight, preferred_element_type=jnp.float32)
        + merge_bias.astype(jnp.float32)
    )
    out_rows = result.astype(jnp.bfloat16)[None]
    grad_low = cotangent[0]
    grad_rows = grad_low.astype(jnp.float32)
    grad_merge_bias = jnp.sum(grad_rows, axis=0)
    grad_merge_weight = jnp.einsum(
        "tc,td->cd", joined, grad_low, preferred_element_type=jnp.float32
    )
    grad_joined = jnp.einsum(
        "td,cd->tc", grad_low, merge_weight, preferred_element_type=jnp.float32
    )
    grad_attn_branch = grad_joined[:, :D].astype(jnp.bfloat16)
    grad_mlp_branch = grad_joined[:, D:].astype(jnp.bfloat16)
    grad_down_weight = jnp.einsum(
        "tc,td->cd", gated_low, grad_mlp_branch, preferred_element_type=jnp.float32
    )
    grad_down_bias = jnp.sum(grad_mlp_branch.astype(jnp.float32), axis=0)
    grad_gated = jnp.einsum(
        "td,cd->tc", grad_mlp_branch, down_weight, preferred_element_type=jnp.float32
    )
    grad_gate_half = grad_gated * conv_out
    grad_conv_out = (grad_gated * gate_half).astype(jnp.bfloat16)
    grad_conv_rows = grad_conv_out.astype(jnp.float32)
    grad_conv_bias = jnp.sum(grad_conv_rows, axis=0)
    grad_wide = extended(grad_conv_out, (("tm", 0),), half_width)
    kernel_list = []
    grad_conv_in = jnp.zeros_like(grad_conv_rows)
    for tap_index in range(KERNEL):
        same_item = (wide_item[tap_index : tap_index + row_count] == item_of)[:, None]
        kernel_list.append(
            jnp.sum(
                jnp.where(
                    same_item, conv_wide[tap_index : tap_index + row_count].astype(jnp.float32), 0.0
                )
                * grad_conv_rows,
                axis=0,
            )
        )
        back_start = 2 * half_width - tap_index
        back_item = (wide_item[back_start : back_start + row_count] == item_of)[:, None]
        grad_conv_in = (
            grad_conv_in
            + jnp.where(
                back_item, grad_wide[back_start : back_start + row_count].astype(jnp.float32), 0.0
            )
            * kernel_rows[tap_index]
        )
    grad_conv_kernel = jnp.stack(kernel_list)
    grad_second, grad_gate_norm_gain, grad_gate_norm_bias = conv_pull(grad_conv_in)
    (grad_pre_rows,) = gelu_pull(jnp.concatenate([grad_gate_half, grad_second], axis=1))
    grad_pre = grad_pre_rows.astype(jnp.bfloat16)
    grad_up_bias = jnp.sum(grad_pre.astype(jnp.float32), axis=0)
    grad_up_weight = jnp.einsum(
        "tc,tf->cf", mlp_norm_low, grad_pre, preferred_element_type=jnp.float32
    )
    grad_mlp_norm = jnp.einsum("tf,cf->tc", grad_pre, up_weight, preferred_element_type=jnp.float32)
    grad_out_weight = jnp.einsum(
        "tc,td->cd", attn_low, grad_attn_branch, preferred_element_type=jnp.float32
    )
    grad_attn_low = jnp.einsum(
        "td,cd->tc", grad_attn_branch, out_weight, preferred_element_type=jnp.float32
    ).astype(jnp.bfloat16)
    grad_out_heads = grad_attn_low.reshape(row_count, HEADS, HEAD)
    delta_rows = jnp.sum(
        jnp.transpose(grad_out_heads.astype(jnp.float32), (1, 0, 2)) * attn_heads, axis=2
    )
    total_frames = row_count * cycle_size
    back_start_state = (
        jnp.zeros((row_count, HEADS, HEAD), jnp.float32),
        jnp.zeros((row_count, HEADS, D), jnp.float32),
        jnp.zeros((total_frames, D), jnp.float32),
        jnp.zeros((total_frames, D), jnp.float32),
    )
    back_key_piece = lax.all_gather(key_rows, "tm", axis=0, tiled=True)
    back_value_piece = lax.all_gather(value_rows, "tm", axis=0, tiled=True)
    extent = back_key_piece.shape[0]
    back_step_rows = step_size(extent)

    def back_one_step(inner_state, step_index):
        grad_content, grad_rel = inner_state
        key_block = lax.dynamic_slice_in_dim(
            back_key_piece, step_index * back_step_rows, back_step_rows, 0
        )
        value_block = lax.dynamic_slice_in_dim(
            back_value_piece, step_index * back_step_rows, back_step_rows, 0
        )
        prob_low, grad_raw, k_rel = block_grads(
            content_heads,
            q_rel,
            item_of,
            frame_index,
            grad_out_heads,
            log_total,
            delta_rows,
            key_block,
            value_block,
            step_index * back_step_rows,
            stream_lengths,
        )
        grad_content = grad_content + jnp.einsum(
            "hqk,khe->qhe",
            grad_raw,
            key_block.reshape(back_step_rows, HEADS, HEAD),
            preferred_element_type=jnp.float32,
        )
        grad_rel = grad_rel + jnp.einsum(
            "hqk,kc->qhc", grad_raw, k_rel, preferred_element_type=jnp.float32
        )
        key_part = jnp.einsum(
            "hqk,qhe->khe", grad_raw, content_heads, preferred_element_type=jnp.float32
        ).reshape(back_step_rows, D)
        value_part = jnp.einsum(
            "hqk,qhe->khe", prob_low, grad_out_heads, preferred_element_type=jnp.float32
        ).reshape(back_step_rows, D)
        return ((grad_content, grad_rel), (key_part, value_part))

    inner_state, block_parts = lax.scan(
        back_one_step,
        (back_start_state[0], back_start_state[1]),
        jnp.arange(extent // back_step_rows, dtype=jnp.int32),
    )
    key_all = block_parts[0].reshape(extent, D)
    value_all = block_parts[1].reshape(extent, D)
    grad_content, grad_rel, key_all, value_all = (
        inner_state[0],
        inner_state[1],
        key_all,
        value_all,
    )
    grad_keys, grad_values = (
        lax.psum_scatter(key_all, "tm", scatter_dimension=0, tiled=True),
        lax.psum_scatter(value_all, "tm", scatter_dimension=0, tiled=True),
    )
    half_size = D // 2
    rel_first = grad_rel[..., :half_size]
    rel_second = grad_rel[..., half_size:]
    sine_wide = sine_rows[:, None, :]
    cosine_wide = cosine_rows[:, None, :]
    grad_projected = jnp.concatenate(
        [
            rel_first * sine_wide - rel_second * cosine_wide,
            rel_first * cosine_wide + rel_second * sine_wide,
        ],
        axis=-1,
    ).astype(jnp.bfloat16)
    grad_pos_weight = jnp.einsum(
        "thc,the->che", grad_projected, position_heads, preferred_element_type=jnp.float32
    ).reshape(D, D)
    grad_q_position = jnp.einsum(
        "thc,che->the", grad_projected, pos_heads, preferred_element_type=jnp.float32
    )
    grad_content_bias = jnp.sum(grad_content, axis=0).reshape(D)
    grad_position_bias = jnp.sum(grad_q_position, axis=0).reshape(D)
    grad_query = (grad_content + grad_q_position).reshape(row_count, D).astype(jnp.bfloat16)
    grad_qkv = jnp.concatenate(
        [grad_query, grad_keys.astype(jnp.bfloat16), grad_values.astype(jnp.bfloat16)], axis=1
    )
    grad_qkv_weight = jnp.einsum(
        "tc,tf->cf", attn_norm_low, grad_qkv, preferred_element_type=jnp.float32
    )
    grad_attn_norm = jnp.einsum(
        "tf,cf->tc", grad_qkv, qkv_weight, preferred_element_type=jnp.float32
    )
    grad_from_attn, grad_ln_attn_gain, grad_ln_attn_bias = attn_pull(grad_attn_norm)
    grad_from_mlp, grad_ln_mlp_gain, grad_ln_mlp_bias = mlp_pull(grad_mlp_norm)
    grad_inputs = grad_rows + grad_from_attn + grad_from_mlp
    weight_grads = (
        grad_ln_attn_gain,
        grad_ln_attn_bias,
        grad_ln_mlp_gain,
        grad_ln_mlp_bias,
        grad_qkv_weight,
        grad_content_bias,
        grad_position_bias,
        grad_pos_weight,
        grad_out_weight,
        grad_up_weight,
        grad_up_bias,
        grad_gate_norm_gain,
        grad_gate_norm_bias,
        grad_conv_kernel,
        grad_conv_bias,
        grad_down_weight,
        grad_down_bias,
        grad_merge_weight,
        grad_merge_bias,
    )
    summed = lax.psum(
        (
            weight_grads[0],
            weight_grads[1],
            weight_grads[2],
            weight_grads[3],
            weight_grads[4],
            weight_grads[5],
            weight_grads[6],
            weight_grads[7],
            weight_grads[8],
            weight_grads[9],
            weight_grads[10],
            weight_grads[11],
            weight_grads[12],
            weight_grads[13],
            weight_grads[14],
            weight_grads[15],
            weight_grads[16],
            weight_grads[17],
            weight_grads[18],
        ),
        "tm",
    )
    shares = (
        lax.psum_scatter(
            summed[0].astype(jnp.bfloat16), "stream", scatter_dimension=0, tiled=True
        ).astype(jnp.float32),
        lax.psum_scatter(
            summed[1].astype(jnp.bfloat16), "stream", scatter_dimension=0, tiled=True
        ).astype(jnp.float32),
        lax.psum_scatter(
            summed[2].astype(jnp.bfloat16), "stream", scatter_dimension=0, tiled=True
        ).astype(jnp.float32),
        lax.psum_scatter(
            summed[3].astype(jnp.bfloat16), "stream", scatter_dimension=0, tiled=True
        ).astype(jnp.float32),
        lax.psum_scatter(
            summed[4].astype(jnp.bfloat16), "stream", scatter_dimension=0, tiled=True
        ).astype(jnp.float32),
        lax.psum_scatter(
            summed[5].astype(jnp.bfloat16), "stream", scatter_dimension=0, tiled=True
        ).astype(jnp.float32),
        lax.psum_scatter(
            summed[6].astype(jnp.bfloat16), "stream", scatter_dimension=0, tiled=True
        ).astype(jnp.float32),
        lax.psum_scatter(
            summed[7].astype(jnp.bfloat16), "stream", scatter_dimension=0, tiled=True
        ).astype(jnp.float32),
        lax.psum_scatter(
            summed[8].astype(jnp.bfloat16), "stream", scatter_dimension=0, tiled=True
        ).astype(jnp.float32),
        lax.psum_scatter(
            summed[9].astype(jnp.bfloat16), "stream", scatter_dimension=0, tiled=True
        ).astype(jnp.float32),
        lax.psum_scatter(
            summed[10].astype(jnp.bfloat16), "stream", scatter_dimension=0, tiled=True
        ).astype(jnp.float32),
        lax.psum_scatter(
            summed[11].astype(jnp.bfloat16), "stream", scatter_dimension=0, tiled=True
        ).astype(jnp.float32),
        lax.psum_scatter(
            summed[12].astype(jnp.bfloat16), "stream", scatter_dimension=0, tiled=True
        ).astype(jnp.float32),
        lax.psum_scatter(
            summed[13].astype(jnp.bfloat16), "stream", scatter_dimension=1, tiled=True
        ).astype(jnp.float32),
        lax.psum_scatter(
            summed[14].astype(jnp.bfloat16), "stream", scatter_dimension=0, tiled=True
        ).astype(jnp.float32),
        lax.psum_scatter(
            summed[15].astype(jnp.bfloat16), "stream", scatter_dimension=0, tiled=True
        ).astype(jnp.float32),
        lax.psum_scatter(
            summed[16].astype(jnp.bfloat16), "stream", scatter_dimension=0, tiled=True
        ).astype(jnp.float32),
        lax.psum_scatter(
            summed[17].astype(jnp.bfloat16), "stream", scatter_dimension=0, tiled=True
        ).astype(jnp.float32),
        lax.psum_scatter(
            summed[18].astype(jnp.bfloat16), "stream", scatter_dimension=0, tiled=True
        ).astype(jnp.float32),
    )
    return (out_rows, grad_inputs[None]) + tuple(shares)


LANES = 128
LOW = LANES // 2
BLOCK = 128
TALL = 256
WINDOW = 64
MARGIN = 16
BOUNDS = 16
MEGA = 1024 * 1024
F32 = jnp.float32
BF16 = jnp.bfloat16


def dot_nn(left, right):
    return jnp.dot(left, right, preferred_element_type=F32)


def dot_nt(left, right):
    return lax.dot_general(left, right, (((1,), (1,)), ((), ())), preferred_element_type=F32)


def dot_tn(left, right):
    return lax.dot_general(left, right, (((0,), (0,)), ((), ())), preferred_element_type=F32)


def rows_of(index, size, base=0):
    return pl.ds(pl.multiple_of(index * size, size) + base, size)


def line_of(ref):
    return ref[...].astype(F32).reshape(1, ref.shape[0])


def fold_rows(values):
    return jnp.sum(values.reshape(values.shape[0] // 8, 8, values.shape[1]), axis=0)


def one_row(values):
    return jnp.sum(values, axis=0, keepdims=True)


def turn(values):
    return pltpu.roll(values, LOW, 1)


def low_lanes(rows):
    return lax.broadcasted_iota(jnp.int32, (rows, LANES), 1) < LOW


def centre_rows(inputs):
    mean = jnp.mean(inputs, axis=-1, keepdims=True)
    centred = inputs - mean
    spread = jnp.mean(centred * centred, axis=-1, keepdims=True)
    return centred * lax.rsqrt(spread + EPS)


def gelu_parts(values):
    phi = 0.5 + 0.5 * lax.erf(values * math.sqrt(0.5))
    bell = jnp.exp(values * values * -0.5)
    return values * phi, phi + values * bell * (1.0 / math.sqrt(2.0 * math.pi))


class Part:
    def __init__(self, shape=None, pairs=None, refs=1, late=False):
        self.shape, self.pairs, self.refs, self.late = shape, pairs, refs, late

    def buffer(self, operand):
        return self.shape or operand.shape

    def copies(self, refs, buffer):
        return self.pairs(refs, buffer) if self.pairs else [(refs[0], buffer)]


def blocks_part():
    def pairs(refs, buffer):
        place = lax.axis_index("tm")
        return [
            (ref, buffer.at[rows_of(lax.bitwise_xor(jnp.int32(apart), place), BLOCK)])
            for apart, ref in enumerate(refs)
        ]

    return Part((HEADS * BLOCK, D), pairs, HEADS)


def rows_part(first, size, late=False):
    return Part((size, D), lambda refs, buffer: [(refs[0].at[pl.ds(first, size)], buffer)], late=late)


class Fetch:
    def __init__(self, pairs, buffer, sems, first):
        self.buffer, self.begun = buffer, False
        self.pending = [
            pltpu.make_async_copy(source, target, sems.at[first + index])
            for index, (source, target) in enumerate(pairs)
        ]

    def begin(self):
        if not self.begun:
            for copy in self.pending:
                copy.start()
        self.begun = True

    def __call__(self):
        self.begin()
        for copy in self.pending:
            copy.wait()
        self.pending = []
        return self.buffer


def begin(*fetches):
    for fetch in fetches:
        fetch.begin()


class Send:
    def __init__(self, buffer, target, sems):
        self.buffer, self.target, self.sems, self.copies = buffer, target, sems, []

    def go(self, *index):
        source, target = (self.buffer.at[index], self.target.at[index]) if index else (self.buffer, self.target)
        copy = pltpu.make_async_copy(source, target, self.sems[len(self.copies)])
        copy.start()
        self.copies.append(copy)

    def finish(self):
        if not self.copies:
            self.go()


SPACES = {"v": pltpu.VMEM, "s": pltpu.SMEM, "k": pl.ANY}


def kernel_call(body, out_shapes, plan, scratch=(), megas=58, bounds=False, aliases=None):
    def call(*operands):
        in_specs, buffers, at = [], [], 0
        for item in plan:
            if item == "f":
                in_specs.append(pl.BlockSpec(memory_space=pl.ANY))
                buffers.append(pltpu.VMEM(operands[at].shape, operands[at].dtype))
                at += 1
            elif isinstance(item, Part):
                in_specs += [pl.BlockSpec(memory_space=pl.ANY)] * item.refs
                buffers.append(pltpu.VMEM(item.buffer(operands[at]), operands[at].dtype))
                at += item.refs
            else:
                in_specs.append(pl.BlockSpec(memory_space=SPACES[item]))
                at += 1
        sent = [out for out in out_shapes if len(out) > 2]
        buffers += [pltpu.VMEM(out[3] if len(out) > 3 else out[0], out[1]) for out in sent]
        sem_count = 96
        extra = [pltpu.SMEM((BOUNDS,), jnp.int32)] if bounds else []

        def outer(*refs):
            inputs, rest = refs[: len(in_specs)], refs[len(in_specs) :]
            outputs, rest = rest[: len(out_shapes)], rest[len(out_shapes) :]
            held, rest = list(rest[: len(buffers)]), rest[len(buffers) :]
            sems, rest = rest[0], rest[1:]
            given, at, used = [], 0, 0
            for item in plan:
                if item == "f":
                    given.append(Fetch([(inputs[at], held[0])], held.pop(0), sems, used))
                    given[-1].begin()
                    used += 1
                    at += 1
                elif isinstance(item, Part):
                    buffer = held.pop(0)
                    pairs = item.copies(inputs[at : at + item.refs], buffer)
                    given.append(Fetch(pairs, buffer, sems, used))
                    if not item.late:
                        given[-1].begin()
                    used += len(pairs)
                    at += item.refs
                else:
                    given.append(inputs[at])
                    at += 1
            results = []
            for out, ref in zip(out_shapes, outputs):
                if len(out) > 2:
                    target = out[4](ref) if len(out) > 3 else ref
                    results.append(Send(held.pop(0), target, [sems.at[used + index] for index in range(4)]))
                    used += 4
                else:
                    results.append(ref)
            assert used <= sem_count
            given = [item() if kind == "f" else item for kind, item in zip(plan, given)]
            body(*given, *results, *rest)
            for item in given:
                if isinstance(item, Fetch):
                    item()
            sends = [item for item in results if isinstance(item, Send)]
            for item in sends:
                item.finish()
            for item in sends:
                for copy in item.copies:
                    copy.wait()

        return pl.pallas_call(
            outer,
            out_shape=[jax.ShapeDtypeStruct(out[0], out[1]) for out in out_shapes],
            in_specs=in_specs,
            out_specs=[pl.BlockSpec(memory_space=pl.ANY if len(out) > 2 else pltpu.VMEM) for out in out_shapes],
            scratch_shapes=buffers
            + [pltpu.SemaphoreType.DMA((sem_count,))]
            + [pltpu.VMEM(shape, kind) for shape, kind in scratch]
            + extra,
            input_output_aliases=aliases or {},
            compiler_params=pltpu.CompilerParams(vmem_limit_bytes=megas * MEGA),
            cost_estimate=pl.CostEstimate(flops=0, bytes_accessed=0, transcendentals=0),
        )(*operands)

    return call


def fill_bounds(lengths_ref, bounds_s, total):
    bounds_s[0] = jnp.int32(0)
    end = jnp.int32(0)
    for item in range(ITEMS):
        end = end + lengths_ref[0, item]
        bounds_s[item + 1] = end
    for item in range(ITEMS + 1, BOUNDS):
        bounds_s[item] = jnp.int32(total)


def select_kernel(
    up_ref,
    up_bias_ref,
    gain_ref,
    bias_ref,
    conv_bias_ref,
    taps_ref,
    qkv_ref,
    pos_ref,
    content_ref,
    position_ref,
    up_out,
    table_out,
    qkv_out,
    pos_out,
    bias_out,
):
    place = lax.axis_index("tm")
    quarters = lax.axis_size("stream")
    share = HALF // (quarters * lax.axis_size("tm"))
    lane = lax.broadcasted_iota(jnp.int32, (1, 2 * LANES), 1)
    channel = jnp.where(lane < LANES + LOW, lane, lane - LOW)
    group = jnp.zeros_like(channel)
    for quarter in range(1, quarters):
        group = group + (channel >= quarter * share).astype(jnp.int32)
    source = group * (HALF // quarters) + share * place + channel - group * share
    chosen = (lax.broadcasted_iota(jnp.int32, (HALF, 2 * LANES), 0) == source).astype(F32).astype(BF16)
    gate = dot_nn(up_ref[:, :HALF], chosen)
    conv = dot_nn(up_ref[:, HALF:], chosen)
    up_out[:, :LANES] = gate[:, :LANES].astype(BF16)
    up_out[:, LANES : 2 * LANES] = jnp.where(low_lanes(D), gate[:, LANES:], conv[:, LANES:]).astype(BF16)
    up_out[:, 2 * LANES :] = conv[:, :LANES].astype(BF16)
    up_bias = line_of(up_bias_ref)
    lines = jnp.concatenate(
        [
            up_bias[:, :HALF],
            up_bias[:, HALF:],
            line_of(gain_ref),
            line_of(bias_ref),
            line_of(conv_bias_ref),
            jnp.zeros((3, HALF), F32),
        ],
        axis=0,
    )
    lines = dot_nn(lines.astype(BF16), chosen)
    taps = dot_nn(taps_ref[...], chosen)
    for part in range(2):
        lanes = slice(part * LANES, (part + 1) * LANES)
        table_out[part, :8] = lines[:, lanes]
        table_out[part, 8 : 8 + KERNEL] = taps[:, lanes]
        table_out[part, 8 + KERNEL :] = jnp.zeros((1, LANES), F32)

    odd = lax.rem(place, 2) == 1

    def head_lanes(ref, base):
        at = pl.ds(pl.multiple_of(lax.div(place, 2) * LANES + base, LANES), LANES)
        values = ref[:, at].astype(F32)
        values = jnp.where(odd, turn(values), values)
        return jnp.where(low_lanes(values.shape[0]), values, 0.0)

    for part in range(3):
        qkv_out[:, part * LANES : (part + 1) * LANES] = head_lanes(qkv_ref, part * D).astype(BF16)
    pos_out[...] = head_lanes(pos_ref, 0).astype(BF16)
    bias_out[...] = jnp.zeros((8, LANES), F32)
    for line, ref in enumerate((content_ref, position_ref)):
        values = line_of(ref)
        picked = values[:, :LANES]
        for tile in range(1, D // LANES):
            picked = jnp.where(
                lax.div(place, 2) == tile, values[:, tile * LANES : (tile + 1) * LANES], picked
            )
        picked = jnp.where(odd, turn(picked), picked)
        bias_out[line : line + 1] = jnp.where(low_lanes(1), picked, 0.0)


def angle_rows(coarse_ref, fine_ref, block, rows):
    half = D // 2
    base = coarse_ref[pl.ds(block, 1)]
    base_sine, base_cosine = base[:, :half], base[:, half:]
    sine, cosine = fine_ref[rows, :half], fine_ref[rows, half:]
    return base_sine * cosine + base_cosine * sine, base_cosine * cosine - base_sine * sine


def item_codes(bounds_s, index):
    code = jnp.zeros_like(index)
    for item in range(1, ITEMS + 1):
        code = code + (index >= bounds_s[item]).astype(jnp.int32)
    return jnp.where(code < ITEMS, code, ITEMS + index)


def attend_kernel(
    lengths_ref,
    x_ref,
    attn_gain_ref,
    attn_bias_ref,
    mlp_gain_ref,
    mlp_bias_ref,
    qkv_ref,
    pos_ref,
    bias_ref,
    coarse_ref,
    fine_ref,
    up_ref,
    up_bias_ref,
    n_attn_out,
    n_mlp_out,
    hat_out,
    q_position_out,
    query_out,
    key_out,
    value_out,
    prob_out,
    attn_out,
    mean_out,
    rate_out,
    bounds_s,
):
    frames = n_attn_out.buffer.shape[0]
    half = D // 2
    fill_bounds(lengths_ref, bounds_s, frames)
    attn_gain, attn_bias = line_of(attn_gain_ref), line_of(attn_bias_ref)
    mlp_gain, mlp_bias = line_of(mlp_gain_ref), line_of(mlp_bias_ref)
    content, position = bias_ref[0:1], bias_ref[1:2]
    x_ref = x_ref()
    begin(up_ref)

    @pl.loop(0, frames // TALL, unroll=4)
    def _(block):
        rows = rows_of(block, TALL)
        for part in range(TALL // 32):
            at = pl.ds(pl.multiple_of(block * TALL + part * 32, 32), 32)
            hat = centre_rows(x_ref[at].astype(F32))
            hat_out.buffer[at] = hat.astype(BF16)
            n_attn_out.buffer[at] = (hat * attn_gain + attn_bias).astype(BF16)
            n_mlp_out.buffer[at] = (hat * mlp_gain + mlp_bias).astype(BF16)
        parts = dot_nn(n_attn_out.buffer[rows], qkv_ref[...])
        query = parts[:, :LANES]
        query_out.buffer[rows, :LANES] = ((query + content).astype(BF16).astype(F32) * 0.125).astype(BF16)
        q_position = (query + position).astype(BF16)
        q_position_out.buffer[rows] = q_position
        key_out.buffer[rows, :LANES] = parts[:, LANES : 2 * LANES].astype(BF16)
        value_out.buffer[rows] = parts[:, 2 * LANES :].astype(BF16)
        projected = dot_nt(q_position, pos_ref[...])
        for part in range(TALL // 32):
            at = pl.ds(pl.multiple_of(block * TALL + part * 32, 32), 32)
            inner = part * 32 % BLOCK
            sine, cosine = angle_rows(
                coarse_ref, fine_ref, block * (TALL // BLOCK) + part * 32 // BLOCK, slice(inner, inner + 32)
            )
            first = projected[part * 32 : part * 32 + 32, :half]
            second = projected[part * 32 : part * 32 + 32, half:]
            query_out.buffer[at, LANES : LANES + half] = ((first * sine + second * cosine) * 0.125).astype(BF16)
            query_out.buffer[at, LANES + half :] = ((second * sine - first * cosine) * 0.125).astype(BF16)
            key_out.buffer[at, LANES : LANES + half] = cosine.astype(BF16)
            key_out.buffer[at, LANES + half :] = sine.astype(BF16)

    for out in (n_attn_out, n_mlp_out, hat_out, q_position_out, query_out, key_out, value_out):
        out.go()
    up_ref = up_ref()
    up_bias = line_of(up_bias_ref)[:, HALF:]
    @pl.loop(0, frames // TALL, unroll=2)
    def _(block):
        values = dot_nn(n_mlp_out.buffer[rows_of(block, TALL)], up_ref[...])
        for part in range(TALL // 16):
            pre = values[part * 16 : part * 16 + 16] + up_bias
            hidden = pre * (0.5 + 0.5 * lax.erf(pre * math.sqrt(0.5)))
            mean = jnp.mean(hidden, axis=-1, keepdims=True)
            centred = hidden - mean
            rate = lax.rsqrt(jnp.mean(centred * centred, axis=-1, keepdims=True) + EPS)
            at = pl.ds(pl.multiple_of(block * TALL + part * 16, 16), 16)
            mean_out.buffer[at] = jnp.broadcast_to(mean, (16, LANES))
            rate_out.buffer[at] = jnp.broadcast_to(rate, (16, LANES))

    mean_out.go()
    rate_out.go()
    key_code = item_codes(bounds_s, lax.broadcasted_iota(jnp.int32, (1, frames), 1))

    low = low_lanes(32)
    for block in range(frames // TALL):
        rows = pl.ds(block * TALL, TALL)
        raw = dot_nt(query_out.buffer[rows], key_out.buffer[...])
        shares = []
        for part in range(TALL // 32):
            start = block * TALL + part * 32
            index = start + lax.broadcasted_iota(jnp.int32, (32, 1), 0)
            scaled = jnp.where(
                item_codes(bounds_s, index) == key_code, raw[part * 32 : part * 32 + 32], MASKED
            )
            weight = jnp.exp(scaled - jnp.max(scaled, axis=1, keepdims=True))
            prob_out.buffer[pl.ds(start, 32)] = weight.astype(BF16)
            shares.append(1.0 / jnp.sum(weight, axis=1, keepdims=True))
        prob_out.go(rows)
        attn = dot_nn(prob_out.buffer[rows], value_out.buffer[...])
        for part in range(TALL // 32):
            share = shares[part]
            attn_out.buffer[pl.ds(block * TALL + part * 32, 32)] = jnp.where(
                low, attn[part * 32 : part * 32 + 32] * share, share
            )


def fill_margins(wide_s, frames):
    edge = jnp.zeros((MARGIN, LANES), F32)
    wide_s[:MARGIN] = edge
    wide_s[MARGIN + frames : 2 * MARGIN + frames] = edge
    base = frames + 3 * MARGIN
    after = base + frames // 2
    low = low_lanes(MARGIN)
    wide_s[base - MARGIN : base] = jnp.where(low, 0.0, turn(wide_s[after - MARGIN : after]))
    wide_s[after : after + MARGIN] = jnp.where(low, turn(wide_s[base : base + MARGIN]), 0.0)


def item_span(bounds_s, frame):
    begin, end = bounds_s[0], bounds_s[BOUNDS - 1]
    for item in range(1, ITEMS + 1):
        edge = bounds_s[item]
        begin = jnp.where(frame >= edge, edge, begin)
    for item in range(ITEMS, 0, -1):
        edge = bounds_s[item]
        end = jnp.where(frame < edge, edge, end)
    return begin, end


def is_whole(bounds_s, start):
    begin, end = item_span(bounds_s, start)
    reach = KERNEL // 2
    low = (begin == 0) | (begin <= start - reach)
    high = (end == bounds_s[BOUNDS - 1]) | (end >= start + WINDOW + reach)
    return low & high & (end >= start + WINDOW)


def tap_limits(bounds_s, start):
    frame = start + lax.broadcasted_iota(jnp.int32, (WINDOW, LANES), 0)
    begin, end = item_span(bounds_s, frame)
    return begin - frame, end - frame


def grouped(values):
    return values.reshape(WINDOW // 8, 8, LANES)


def triple_places(step, frames):
    half = frames // 2
    return (
        pl.multiple_of(step * WINDOW, 2 * MARGIN),
        pl.multiple_of(step * WINDOW + half, 2 * MARGIN),
        pl.multiple_of(step * WINDOW + frames + 2 * MARGIN, 2 * MARGIN),
    )


def over_windows(bounds_s, frames, body):
    half = frames // 2

    @pl.loop(0, half // WINDOW)
    def _(step):
        start = step * WINDOW
        whole = is_whole(bounds_s, start) & is_whole(bounds_s, start + half)

        @pl.when(whole)
        def _():
            body(step, (0, 1, 2), None)

        @pl.when(jnp.logical_not(whole))
        def _():
            first, second = tap_limits(bounds_s, start), tap_limits(bounds_s, start + half)
            low = low_lanes(WINDOW)
            body(step, (2,), [jnp.where(low, one, other) for one, other in zip(first, second)])
            for index, own, limits in ((0, start, first), (1, start + half, second)):
                alone = is_whole(bounds_s, own)

                @pl.when(alone)
                def _(index=index):
                    body(step, (index,), None)

                @pl.when(jnp.logical_not(alone))
                def _(index=index, limits=limits):
                    body(step, (index,), limits)


def tap_mask(tap, limits):
    shift = tap - KERNEL // 2
    return None if limits is None else (limits[0] <= shift) & (limits[1] > shift)


def tap_view(window_ref, tap, mask):
    view = window_ref[tap + 1 : tap + 1 + WINDOW]
    return grouped(view if mask is None else jnp.where(mask, view, 0.0))


def mlp_first_kernel(
    lengths_ref,
    n_ref,
    up_ref,
    table_ref,
    mean_ref,
    rate_ref,
    cot_ref,
    merge_ref,
    down_ref,
    attn_ref,
    mixed_out,
    gate_pre_out,
    grad_out,
    rate_out,
    hat_out,
    early_out,
    vectors_out,
    lines_out,
    hat_s,
    slope_s,
    gate_s,
    hidden_s,
    gate_slope_s,
    conv_s,
    grad_s,
    out_s,
    back_s,
    branch_s,
    mix_s,
    taps_s,
    turn_s,
    tap_sum_s,
    columns_s,
    forward_s,
    backward_s,
    bounds_s,
):
    place = lax.axis_index("tm")
    frames = mix_s.shape[0]
    half = frames // 2
    blocks = frames // BLOCK
    quarters, early_rows, _ = early_out.buffer.shape
    share = early_rows // 8
    channels = quarters * share
    fill_bounds(lengths_ref, bounds_s, frames)
    for part in range(2):
        for tap in range(KERNEL):
            line = jnp.broadcast_to(table_ref[part, 8 + tap : 9 + tap], (8, LANES))
            taps_s[part, tap] = line
            turn_s[part, KERNEL - 1 - tap] = line
    tap_sum_s[...] = jnp.zeros(tap_sum_s.shape, F32)
    main, rest = table_ref[0, :8], table_ref[1, :8]
    mixed_bias = jnp.where(low_lanes(1), rest[0:1], rest[1:2])
    low = low_lanes(64)
    gate_pre_ref = gate_pre_out.buffer
    n_ref = n_ref()
    mean_ref, rate_ref = mean_ref(), rate_ref()
    begin(cot_ref, merge_ref, down_ref, attn_ref)

    def stat_rows(rows):
        return mean_ref[rows], rate_ref[rows]

    def chunk(start, base=0):
        return pl.ds(pl.multiple_of(start, 64) + base, 64)

    def conv_part(hidden, mean, rate, lines, rows, to_rows):
        hat = (hidden - mean) * rate
        hat_s[rows] = hat
        hat_out.buffer[rows] = hat.astype(BF16)
        conv_s[to_rows] = (hat * lines[2:3] + lines[3:4]).astype(BF16).astype(F32)

    @pl.loop(0, half // TALL, unroll=2)
    def _(block):
        pre = [dot_nn(n_ref[rows_of(block, TALL, base)], up_ref[...]) for base in (0, half)]
        for part in range(TALL // 64):
            inner = slice(part * 64, part * 64 + 64)
            start = block * TALL + part * 64
            mixed = []
            for values, base in zip(pre, (0, half)):
                rows = chunk(start, base)
                gate, gate_slope = gelu_parts(values[inner, :LANES] + main[0:1])
                hidden_s[rows] = gate
                gate_slope_s[rows] = gate_slope
                hidden, slope = gelu_parts(values[inner, 2 * LANES :] + main[1:2])
                mean, rate = stat_rows(rows)
                slope_s[rows] = slope * rate
                conv_part(hidden, mean, rate, main, rows, chunk(start, base + MARGIN))
                mixed.append((*gelu_parts(values[inner, LANES : 2 * LANES] + mixed_bias), mean, rate))
            (low_hidden, low_slope, low_mean, low_rate), (high_hidden, high_slope, high_mean, high_rate) = mixed
            rows = chunk(start, frames)
            hidden_s[rows] = jnp.where(low, low_hidden, turn(high_hidden))
            gate_slope_s[rows] = jnp.where(low, low_slope, turn(high_slope))
            rate = jnp.where(low, low_rate, high_rate)
            slope_s[rows] = jnp.where(low, turn(low_slope), high_slope) * rate
            conv_part(
                jnp.where(low, turn(low_hidden), high_hidden),
                jnp.where(low, low_mean, high_mean),
                rate,
                rest,
                rows,
                chunk(start, frames + 3 * MARGIN),
            )

    hat_out.go()
    fill_margins(conv_s, frames)
    tall = WINDOW + 2 * MARGIN
    outs = (0, half, frames)

    def convolve(step, indices, limits):
        bases = triple_places(step, frames)
        for index in indices:
            forward_s[index] = conv_s[pl.ds(bases[index], tall)]
        for index in indices:
            total = jnp.zeros((WINDOW // 8, 8, LANES), F32)
            for tap in range(KERNEL):
                mask = tap_mask(tap, limits)
                total = total + tap_view(forward_s.at[index], tap, mask) * taps_s[index // 2, tap][None]
            lines = rest if index == 2 else main
            out_s[rows_of(step, WINDOW, outs[index])] = total.reshape(WINDOW, LANES) + lines[4:5]

    over_windows(bounds_s, frames, convolve)
    cot_ref = cot_ref()
    merge_ref = merge_ref()
    down_ref = down_ref()
    attn_ref = attn_ref()
    down_ref[channels:] = jnp.zeros((2 * LANES - channels, D), BF16)
    zero = jnp.zeros((8, LANES), F32)

    def branch_part(grad_gated, rows, to_rows, sums):
        up_sum, conv_sum = sums
        gate, conv = hidden_s[rows], out_s[rows]
        gate_pre = (grad_gated * conv * gate_slope_s[rows]).astype(BF16)
        gate_pre_ref[rows] = gate_pre
        grad_conv = (grad_gated * gate).astype(BF16).astype(F32)
        grad_s[to_rows] = grad_conv
        gate_pre = gate_pre.astype(F32)
        return gate * conv, gate_pre, (up_sum + fold_rows(gate_pre), conv_sum + fold_rows(grad_conv))

    def branch_step(block, sums):
        main_sums, rest_sums = sums
        grads = []
        for base in (0, half):
            rows = rows_of(block, TALL, base)
            branch = dot_nt(cot_ref[rows], merge_ref[...]).astype(BF16)
            branch_s[rows] = branch
            grads.append(dot_nt(branch, down_ref[...]))
        for part in range(TALL // 64):
            inner = slice(part * 64, part * 64 + 64)
            start = block * TALL + part * 64
            for values, base in zip(grads, (0, half)):
                rows = chunk(start, base)
                gated, gate_pre, main_sums = branch_part(
                    values[inner, :LANES], rows, chunk(start, base + MARGIN), main_sums
                )
                mix_s[rows, :LANES] = gated.astype(BF16)
                gate_s[rows, :LANES] = gate_pre.astype(BF16)
            grad = jnp.where(low, grads[0][inner, LANES:], turn(grads[1][inner, LANES:]))
            gated, gate_pre, rest_sums = branch_part(
                grad, chunk(start, frames), chunk(start, frames + 3 * MARGIN), rest_sums
            )
            low_rows, high_rows = chunk(start), chunk(start, half)
            gate_s[low_rows, LANES:] = gate_pre.astype(BF16)
            gate_s[high_rows, LANES:] = turn(gate_pre).astype(BF16)
            mix_s[low_rows, LANES:] = jnp.where(low, gated, turn(attn_ref[low_rows])).astype(BF16)
            mix_s[high_rows, LANES:] = jnp.where(low, turn(gated), turn(attn_ref[high_rows])).astype(BF16)
        return main_sums, rest_sums

    (main_up, main_conv), (rest_up, rest_conv) = lax.fori_loop(
        0, half // TALL, branch_step, ((zero, zero), (zero, zero)), unroll=2
    )
    gate_pre_out.go()
    fill_margins(grad_s, frames)
    own = rows_of(place, BLOCK)
    lines_out[0:1] = one_row(fold_rows(branch_s[own].astype(F32)))
    lines_out[1:2] = one_row(fold_rows(cot_ref[own].astype(F32)))
    lines_out[2:8] = jnp.zeros((6, D), F32)
    grad_down = dot_tn(mix_s[...], branch_s[...])
    grad_gate = dot_tn(gate_s[...], n_ref[...])
    for quarter in range(quarters):
        for tile in range(4):
            early_out.buffer[quarter, tile * share : (tile + 1) * share] = grad_down[
                quarter * share : (quarter + 1) * share, tile * LANES : (tile + 1) * LANES
            ].astype(BF16)
        early_out.buffer[quarter, 4 * share :] = grad_gate[
            :channels, quarter * LANES : (quarter + 1) * LANES
        ].astype(BF16)
    early_out.go()
    for block in range(blocks):
        mixed_out.buffer[block, :BLOCK] = mix_s[block * BLOCK : (block + 1) * BLOCK]
    mixed_out.go(slice(None), pl.ds(0, BLOCK))

    def differentiate(step, indices, limits):
        bases = triple_places(step, frames)
        for index in indices:
            forward_s[index] = conv_s[pl.ds(bases[index], tall)]
            backward_s[index] = grad_s[pl.ds(bases[index], tall)]
        for index in indices:
            total = jnp.zeros((WINDOW // 8, 8, LANES), F32)
            centre = grouped(backward_s[index, MARGIN : MARGIN + WINDOW])
            for tap in range(KERNEL):
                mask = tap_mask(tap, limits)
                total = total + tap_view(backward_s.at[index], tap, mask) * turn_s[index // 2, tap][None]
                tap_sum_s[index // 2, tap] += jnp.sum(tap_view(forward_s.at[index], tap, mask) * centre, axis=0)
            back_s[rows_of(step, WINDOW, outs[index])] = total.reshape(WINDOW, LANES)

    over_windows(bounds_s, frames, differentiate)
    lane = lax.broadcasted_iota(jnp.int32, (64, LANES), 1)

    def norm_part(rows, lines, sums):
        gain_sum, bias_sum = sums
        back, hat, slope = back_s[rows], hat_s[rows], slope_s[rows]
        grad = back * lines[2:3]
        grad_out.buffer[rows] = (grad * slope).astype(BF16)
        rate_out.buffer[rows] = slope.astype(BF16)
        along = back * hat
        return grad, along * lines[2:3], (gain_sum + fold_rows(along), bias_sum + fold_rows(back))

    def norm_step(block, sums):
        main_sums, rest_sums = sums
        for part in range(TALL // 64):
            start = block * TALL + part * 64
            pairs = []
            for base in (0, half):
                plain, along, main_sums = norm_part(chunk(start, base), main, main_sums)
                pairs.append([plain, along])
            plain, along, rest_sums = norm_part(chunk(start, frames), rest, rest_sums)
            for item, values in enumerate((plain, along)):
                pairs[0][item] = pairs[0][item] + jnp.where(low, values, 0.0)
                pairs[1][item] = pairs[1][item] + jnp.where(low, 0.0, values)
            for (plain, along), base in zip(pairs, (0, half)):
                columns_s[chunk(start, base)] = jnp.where(
                    lane == 0,
                    jnp.sum(plain, axis=-1, keepdims=True),
                    jnp.where(lane == 1, jnp.sum(along, axis=-1, keepdims=True), 0.0),
                )
        return main_sums, rest_sums

    (main_gain, main_bias), (rest_gain, rest_bias) = lax.fori_loop(
        0, half // TALL, norm_step, ((zero, zero), (zero, zero)), unroll=2
    )
    grad_out.go()
    rate_out.go()
    totals = jnp.concatenate(
        [jnp.transpose(columns_s[block * BLOCK : (block + 1) * BLOCK])[:2] for block in range(blocks)], axis=0
    )
    high = totals.astype(BF16)
    low_part = (totals - high.astype(F32)).astype(BF16)
    for block in range(blocks):
        mixed_out.buffer[block, BLOCK:, :LANES] = high
        mixed_out.buffer[block, BLOCK:, LANES:] = low_part
    mixed_out.go(slice(None), pl.ds(BLOCK, 2 * blocks))

    def vectors(part, lines):
        taps = jnp.sum(tap_sum_s[part], axis=1)[:KERNEL]
        stacked = jnp.concatenate([taps] + [one_row(line) for line in lines], axis=0)
        if part:
            stacked = stacked + turn(stacked)
        return jnp.transpose(
            jnp.concatenate([stacked, jnp.zeros((LANES - stacked.shape[0], LANES), F32)], axis=0)
        )

    vectors_out[:LANES] = vectors(0, (main_conv, main_gain, main_bias, main_up))
    vectors_out[LANES:] = vectors(1, (rest_conv, rest_gain, rest_bias, rest_up))[: channels - LANES]


def attend_back_kernel(
    cot_ref,
    merge_ref,
    head_ref,
    attn_ref,
    value_ref,
    prob_ref,
    key_ref,
    coarse_ref,
    fine_ref,
    pos_ref,
    query_ref,
    n_ref,
    q_position_ref,
    qkv_ref,
    hat_ref,
    gain_ref,
    early_ref,
    branch_out,
    total_out,
    pack_0,
    pack_1,
    pack_2,
    pack_3,
    lines_out,
    grad_s,
    raw_s,
    projected_s,
    parts_s,
    grads_s,
):
    place = lax.axis_index("tm")
    frames = raw_s.shape[0]
    blocks = frames // BLOCK
    half = D // 2
    zero = jnp.zeros((8, LANES), F32)
    cot_ref, merge_ref, head_ref, attn_ref = cot_ref(), merge_ref(), head_ref(), attn_ref()
    head_ref[HEAD:] = jnp.zeros((LANES - HEAD, D), BF16)
    begin(value_ref, prob_ref, key_ref, pos_ref)

    @pl.loop(0, frames // TALL, unroll=4)
    def _(block):
        rows = rows_of(block, TALL)
        branch = dot_nt(cot_ref[rows], merge_ref[...]).astype(BF16)
        branch_out.buffer[rows] = branch
        grad_s[rows] = (dot_nt(branch, head_ref[...]) * attn_ref[rows, HEAD : HEAD + 1]).astype(BF16)

    branch_out.go()
    value_ref, prob_ref = value_ref(), prob_ref()
    key_ref, pos_ref = key_ref(), pos_ref()
    begin(query_ref, n_ref, q_position_ref, qkv_ref, hat_ref, early_ref)

    def score_step(block, sums):
        content_sum, position_sum = sums
        rows = rows_of(block, TALL)
        grad = grad_s[rows]
        score = dot_nt(grad, value_ref[...])
        for part in range(TALL // 32):
            at = pl.ds(pl.multiple_of(block * TALL + part * 32, 32), 32)
            inner = slice(part * 32, part * 32 + 32)
            delta = jnp.sum(grad[inner].astype(F32) * attn_ref[at], axis=1, keepdims=True)
            raw_s[at] = (prob_ref[at].astype(F32) * (score[inner] - delta)).astype(BF16)
        query = dot_nn(raw_s[rows], key_ref[...]) * 0.125
        for part in range(TALL // 32):
            at = pl.ds(pl.multiple_of(block * TALL + part * 32, 32), 32)
            inner = part * 32 % BLOCK
            sine, cosine = angle_rows(
                coarse_ref, fine_ref, block * (TALL // BLOCK) + part * 32 // BLOCK, slice(inner, inner + 32)
            )
            inner = slice(part * 32, part * 32 + 32)
            first, second = query[inner, LANES : LANES + half], query[inner, LANES + half :]
            projected_s[at, :half] = (first * sine - second * cosine).astype(BF16)
            projected_s[at, half:] = (first * cosine + second * sine).astype(BF16)
        position = dot_nn(projected_s[rows], pos_ref[...])
        content = query[:, :LANES]
        parts_s[rows, :LANES] = (content + position).astype(BF16)
        return content_sum + fold_rows(content), position_sum + fold_rows(position)

    content_sum, position_sum = lax.fori_loop(0, frames // TALL, score_step, (zero, zero), unroll=4)
    query_ref, n_ref, q_position_ref = query_ref(), n_ref(), q_position_ref()
    qkv_ref, hat_ref = qkv_ref(), hat_ref()
    grad_key = dot_tn(query_ref[...], raw_s[...])
    grad_value = dot_tn(grad_s[...], prob_ref[...])
    for block in range(blocks):
        at = slice(block * BLOCK, (block + 1) * BLOCK)
        parts_s[at, LANES : 2 * LANES] = jnp.transpose(grad_key[:, at]).astype(BF16)
        parts_s[at, 2 * LANES :] = jnp.transpose(grad_value[:, at]).astype(BF16)
    grads_s[:HEAD] = dot_tn(parts_s[:, :LANES], n_ref[...])[:HEAD]
    grads_s[HEAD : 2 * HEAD] = dot_nn(grad_key.astype(BF16), n_ref[...])[:HEAD]
    grads_s[2 * HEAD : 3 * HEAD] = dot_nn(grad_value.astype(BF16), n_ref[...])[:HEAD]
    grads_s[3 * HEAD :] = dot_tn(q_position_ref[...], projected_s[...])[:HEAD]
    stream = lax.axis_index("stream")
    early_ref = early_ref()
    for apart, pack_out in enumerate((pack_0, pack_1, pack_2, pack_3)):
        quarter = lax.bitwise_xor(stream, jnp.int32(apart))
        lanes = pl.ds(pl.multiple_of(quarter * LANES, LANES), LANES)
        pack_out.buffer[: 4 * HEAD] = grads_s[:, lanes].astype(BF16)
        pack_out.buffer[4 * HEAD :] = early_ref[quarter]
        pack_out.go()
    gain = line_of(gain_ref)
    wide_zero = jnp.zeros((8, D), F32)

    def norm_step(block, sums):
        gain_sum, bias_sum = sums
        grad = dot_nt(parts_s[rows_of(block, TALL)], qkv_ref[...])
        for part in range(TALL // 32):
            at = pl.ds(pl.multiple_of(block * TALL + part * 32, 32), 32)
            own = grad[part * 32 : part * 32 + 32]
            total_out.buffer[at] = (own * gain).astype(BF16)
            gain_sum = gain_sum + fold_rows(own * hat_ref[at].astype(F32))
            bias_sum = bias_sum + fold_rows(own)
        return gain_sum, bias_sum

    gain_sum, bias_sum = lax.fori_loop(0, frames // TALL, norm_step, (wide_zero, wide_zero), unroll=4)
    lane = lax.broadcasted_iota(jnp.int32, (1, LANES), 1)

    def own_lanes(sums):
        line = one_row(sums)
        line = line + turn(line)
        tiles = [
            jnp.where(lax.div(tile * LANES + lane, HEAD) == place, line, 0.0) for tile in range(D // LANES)
        ]
        return jnp.concatenate(tiles, axis=1)

    lines_out[...] = jnp.concatenate(
        [
            one_row(gain_sum),
            one_row(bias_sum),
            own_lanes(content_sum),
            own_lanes(position_sum),
            jnp.zeros((4, D), F32),
        ],
        axis=0,
    )


def mlp_second_kernel(
    mixed_ref,
    gate_pre_ref,
    grad_ref,
    rate_ref,
    hat_ref,
    up_ref,
    norm_hat_ref,
    gain_ref,
    other_ref,
    pre_out,
    same_out,
    apart_out,
    lines_out,
    up_out,
    columns_s,
):
    place = lax.axis_index("tm")
    pre_s = pre_out.buffer
    frames = pre_s.shape[0]
    half = frames // 2
    blocks = frames // BLOCK
    totals = jnp.zeros((2 * blocks, LANES), F32)
    mixed_ref = mixed_ref()
    for source in range(mixed_ref.shape[0]):
        both = mixed_ref[source].astype(F32)
        totals = totals + (both[:, :LANES] + both[:, LANES:])
    totals = totals * (1.0 / HALF)
    high = totals.astype(BF16)
    low_part = (totals - high.astype(F32)).astype(BF16)
    both = jnp.concatenate([high, low_part], axis=0)
    lane = lax.broadcasted_iota(jnp.int32, (4 * blocks, 2 * LANES), 1) // LANES
    line = lax.broadcasted_iota(jnp.int32, (4 * blocks, 2 * LANES), 0)
    for block in range(blocks):
        chosen = (lax.rem(line, 2 * blocks) == 2 * block + lane).astype(F32).astype(BF16)
        columns_s[block * BLOCK : (block + 1) * BLOCK] = dot_tn(both, chosen)
    gate_pre_ref, grad_ref, rate_ref, hat_ref = gate_pre_ref(), grad_ref(), rate_ref(), hat_ref()
    begin(up_ref, norm_hat_ref, other_ref)
    low = low_lanes(64)
    gain = line_of(gain_ref)

    def chunk(start, base=0):
        return pl.ds(pl.multiple_of(start, 64) + base, 64)

    def pre_part(rows, table, up_sum):
        plain, along = table
        hat, rate = hat_ref[rows].astype(F32), rate_ref[rows].astype(F32)
        pre = (grad_ref[rows].astype(F32) - rate * (plain + hat * along)).astype(BF16).astype(F32)
        return pre, up_sum + fold_rows(pre)

    def pre_step(block, sums):
        main_up, rest_up = sums
        for part in range(TALL // 64):
            start = block * TALL + part * 64
            tables = []
            for base in (0, half):
                rows = chunk(start, base)
                table = [columns_s[rows, item * LANES : (item + 1) * LANES] for item in range(2)]
                tables.append(table)
                pre, main_up = pre_part(rows, table, main_up)
                pre_s[rows, :LANES] = gate_pre_ref[rows]
                pre_s[rows, 2 * LANES :] = pre.astype(BF16)
            rows = chunk(start, frames)
            table = [jnp.where(low, one, other) for one, other in zip(*tables)]
            pre, rest_up = pre_part(rows, table, rest_up)
            gate_pre = gate_pre_ref[rows].astype(F32)
            pre_s[chunk(start), LANES : 2 * LANES] = jnp.where(low, gate_pre, turn(pre)).astype(BF16)
            pre_s[chunk(start, half), LANES : 2 * LANES] = jnp.where(low, turn(gate_pre), pre).astype(BF16)
        return main_up, rest_up

    zero = jnp.zeros((8, LANES), F32)
    main_up, rest_up = lax.fori_loop(0, half // TALL, pre_step, (zero, zero), unroll=2)
    pre_out.go()
    up_ref, norm_hat_ref, other_ref = up_ref(), norm_hat_ref(), other_ref()
    wide_zero = jnp.zeros((8, D), F32)

    def norm_step(step, sums):
        gain_sum, bias_sum = sums
        grads = dot_nt(pre_s[rows_of(step, TALL)], up_ref[...])
        for part in range(TALL // BLOCK):
            block = step * (TALL // BLOCK) + part
            rows = rows_of(block, BLOCK)
            grad = grads[part * BLOCK : (part + 1) * BLOCK]
            total = (grad * gain + other_ref[rows].astype(F32)).astype(BF16)
            apart = lax.bitwise_xor(block, place)

            @pl.when(lax.rem(apart, 2) == 0)
            def _(apart=apart, total=total):
                same_out.buffer[lax.div(apart, 2)] = total

            @pl.when(lax.rem(apart, 2) == 1)
            def _(apart=apart, total=total):
                apart_out.buffer[lax.div(apart, 2)] = total

            gain_sum = gain_sum + fold_rows(grad * norm_hat_ref[rows].astype(F32))
            bias_sum = bias_sum + fold_rows(grad)
        return gain_sum, bias_sum

    gain_sum, bias_sum = lax.fori_loop(0, frames // TALL, norm_step, (wide_zero, wide_zero), unroll=2)
    apart_out.go()
    same_out.go()
    lines_out[...] = jnp.concatenate([one_row(gain_sum), one_row(bias_sum), jnp.zeros((6, D), F32)], axis=0)
    rest_line = one_row(rest_up)
    up_out[:LANES] = jnp.transpose(jnp.broadcast_to(one_row(main_up), (LANES, LANES)))
    up_out[LANES:] = jnp.transpose(jnp.broadcast_to(rest_line + turn(rest_line), (LANES, LANES)))[:LOW]


def late_pack_kernel(
    pre_ref,
    n_ref,
    joined_ref,
    branch_ref,
    cot_ref,
    vectors_ref,
    up_columns_ref,
    first_lines_ref,
    head_lines_ref,
    own_lines_ref,
    pack_out,
):
    pack_ref = pack_out.buffer
    quarters = pack_ref.shape[0]
    channels = vectors_ref.shape[0]
    share = channels // quarters
    gate_at = KERNEL + 3
    lane = lax.broadcasted_iota(jnp.int32, (share, LANES), 1)
    lines = jnp.concatenate(
        [
            head_lines_ref[0:2],
            own_lines_ref[0:2],
            head_lines_ref[2:4],
            first_lines_ref[0:2],
            jnp.zeros((8, D), F32),
        ],
        axis=0,
    )
    for quarter in range(quarters):
        table = vectors_ref[quarter * share : (quarter + 1) * share]
        for other in range(2):
            at = slice((2 * (quarter % 2) + other) * share, (2 * (quarter % 2) + other + 1) * share)
            column = vectors_ref[at, gate_at : gate_at + 1] if quarter < quarters // 2 else up_columns_ref[at, 0:1]
            table = jnp.where(lane == gate_at + other, column, table)
        pack_ref[quarter, channels : channels + share] = table.astype(BF16)
        pack_ref[quarter, channels + share : channels + share + 16] = lines[
            :, quarter * LANES : (quarter + 1) * LANES
        ].astype(BF16)
    grad_up = dot_tn(pre_ref()[...], n_ref()[...])
    for quarter in range(quarters):
        lanes = slice(quarter * LANES, (quarter + 1) * LANES)
        pack_ref[quarter, :LANES] = grad_up[LANES:, lanes].astype(BF16)
        pack_ref[quarter, LANES:channels] = grad_up[LOW:LANES, lanes].astype(BF16)
    joined_ref, cot_ref, branch_ref = joined_ref(), cot_ref(), branch_ref()
    sources, _, rows = joined_ref.shape
    merge_rows = 2 * D // sources
    head_rows = D // sources
    grad_merge = jnp.zeros((merge_rows, D), F32)
    grad_head = jnp.zeros((head_rows, D), F32)
    for source in range(sources):
        at = slice(source * rows, (source + 1) * rows)
        joined = joined_ref[source]
        grad_merge = grad_merge + dot_nn(joined[:merge_rows], cot_ref[at])
        grad_head = grad_head + dot_nn(joined[merge_rows : merge_rows + head_rows], branch_ref[at])
    for quarter in range(quarters):
        base = channels + share + 16
        for grad in (grad_merge, grad_head):
            part = grad.shape[0] // quarters
            for tile in range(4):
                pack_ref[quarter, base : base + part] = grad[
                    quarter * part : (quarter + 1) * part, tile * LANES : (tile + 1) * LANES
                ].astype(BF16)
                base += part


def output_kernel(
    x_ref, mixed_ref, head_ref, down_ref, down_bias_ref, merge_ref, merge_bias_ref, out_ref, joined_out
):
    sources = mixed_ref.shape[0]
    rows = x_ref.shape[0]
    channels = HALF // sources
    share = channels // 4
    attn_parts = []
    branch_attn = jnp.zeros((rows, D), F32)
    branch_mlp = jnp.zeros((rows, D), F32)
    for source in range(sources):
        attn = turn(mixed_ref[source, :rows, LANES:].astype(F32))[:, :HEAD].astype(BF16)
        attn_parts.append(attn)
        branch_attn = branch_attn + dot_nn(attn, head_ref[source * HEAD : (source + 1) * HEAD])
        down = jnp.concatenate(
            [down_ref[(part * sources + source) * share : (part * sources + source + 1) * share] for part in range(4)],
            axis=0,
        )
        branch_mlp = branch_mlp + dot_nn(mixed_ref[source, :rows, :channels], down)
    joined = jnp.concatenate(
        [branch_attn.astype(BF16), (branch_mlp + line_of(down_bias_ref)).astype(BF16)], axis=1
    )
    result = x_ref[...].astype(F32) + dot_nn(joined, merge_ref[...]) + line_of(merge_bias_ref)
    out_ref[...] = result.astype(BF16)
    turned = jnp.transpose(joined.astype(F32))
    heads = jnp.transpose(jnp.concatenate(attn_parts, axis=1).astype(F32))
    merge_share = turned.shape[0] // (4 * sources)
    head_share = heads.shape[0] // (4 * sources)
    used = 4 * (merge_share + head_share)
    for target in range(sources):
        for part in range(4):
            at = (part * sources + target) * merge_share
            joined_out[target, part * merge_share : (part + 1) * merge_share] = turned[
                at : at + merge_share
            ].astype(BF16)
            at = (part * sources + target) * head_share
            to = 4 * merge_share + part * head_share
            joined_out[target, to : to + head_share] = heads[at : at + head_share].astype(BF16)
        joined_out[target, used:] = jnp.zeros((joined_out.shape[1] - used, rows), BF16)


def pair_kernel(same_ref, other_ref, *out_refs):
    for slot, out_ref in enumerate(out_refs):
        out_ref[...] = (same_ref[slot].astype(F32) + other_ref[slot].astype(F32)).astype(BF16)


def frames_kernel(x_ref, cot_ref, *refs):
    total_refs, out_ref = refs[:-1], refs[-1]
    for part in range(x_ref.shape[0] // 32):
        rows = slice(part * 32, part * 32 + 32)
        inputs = x_ref[rows].astype(F32)
        mean = jnp.mean(inputs, axis=-1, keepdims=True)
        centred = inputs - mean
        rate = lax.rsqrt(jnp.mean(centred * centred, axis=-1, keepdims=True) + EPS)
        hat = centred * rate
        grad = total_refs[0][rows].astype(F32)
        for total_ref in total_refs[1:]:
            grad = grad + total_ref[rows].astype(F32)
        plain = jnp.mean(grad, axis=-1, keepdims=True)
        along = jnp.mean(grad * hat, axis=-1, keepdims=True)
        out_ref[rows] = cot_ref[rows].astype(F32) + rate * (grad - plain - hat * along)


def add_kernel(*refs):
    out_ref = refs[-1]
    first = 0
    for at in range(0, len(refs) - 1, 4):
        total = refs[at][...].astype(F32)
        for ref in refs[at + 1 : at + 4]:
            total = total + ref[...].astype(F32)
        out_ref[first : first + total.shape[0]] = total.astype(BF16)
        first += total.shape[0]


def gather_parts(near_ref, far_ref, all_s):
    place = lax.axis_index("tm")
    for apart in range(all_s.shape[0]):
        part_ref = far_ref if apart % 2 else near_ref
        all_s[lax.bitwise_xor(jnp.int32(apart), place)] = part_ref[apart // 2]


def lines_from(all_s, base, size):
    return jnp.concatenate([all_s[source, base : base + size] for source in range(all_s.shape[0])], axis=0).astype(F32)


def add_streams_kernel(parts_ref, out_ref):
    total = parts_ref[0].astype(F32)
    for source in range(1, parts_ref.shape[0]):
        total = total + parts_ref[source].astype(F32)
    out_ref[...] = total.astype(BF16)


def early_kernel(near_ref, far_ref, qkv_out, pos_out, down_out, up_out, all_s):
    gather_parts(near_ref, far_ref, all_s)
    sources = all_s.shape[0]
    share = HALF // (4 * sources)
    for kind in range(4):
        lines = jnp.transpose(lines_from(all_s, kind * HEAD, HEAD))
        if kind < 3:
            qkv_out[:, kind * D : (kind + 1) * D] = lines
        else:
            pos_out[...] = lines
    base = 4 * HEAD
    for source in range(sources):
        for tile in range(4):
            down_out[source * share : (source + 1) * share, tile * LANES : (tile + 1) * LANES] = all_s[
                source, base + tile * share : base + (tile + 1) * share
            ].astype(F32)
    wide = sources * share
    for group in range(4):
        up_out.buffer[:, group * wide : (group + 1) * wide] = jnp.transpose(
            lines_from(all_s, base + 4 * share + group * share, share)
        )


def late_kernel(*refs):
    _, near_ref, far_ref = refs[:3]
    (
        attn_gain_out,
        attn_bias_out,
        mlp_gain_out,
        mlp_bias_out,
        content_out,
        position_out,
        outw_out,
        up_out,
        up_bias_out,
        gain_out,
        bias_out,
        taps_out,
        conv_bias_out,
        down_bias_out,
        merge_out,
        merge_bias_out,
        all_s,
    ) = refs[3:]
    gather_parts(near_ref, far_ref, all_s)
    sources = all_s.shape[0]
    channels = HALF // sources
    share = channels // 4
    base = 0
    for group in range(4):
        at = group * sources * share
        up_out.buffer[:, at : at + sources * share] = jnp.transpose(lines_from(all_s, base + group * share, share))
    up_out.go()
    table = jnp.transpose(lines_from(all_s, base + channels, share))
    taps_out[...] = table[:KERNEL]
    conv_bias_out[...] = table[KERNEL]
    gain_out[...] = table[KERNEL + 1]
    bias_out[...] = table[KERNEL + 2]
    wide = sources * share
    up_bias_out[:wide] = table[KERNEL + 3]
    up_bias_out[wide:] = table[KERNEL + 4]
    base = base + channels + share
    lines = all_s[0, base : base + 16].astype(F32)
    for source in range(1, sources):
        lines = lines + all_s[source, base : base + 16].astype(F32)
    outs = (attn_gain_out, attn_bias_out, mlp_gain_out, mlp_bias_out, content_out, position_out, down_bias_out, merge_bias_out)
    for line, out in enumerate(outs):
        out[...] = lines[line]
    base = base + 16
    merge_share = 2 * D // (4 * sources)
    head_share = D // (4 * sources)
    for source in range(sources):
        for tile in range(4):
            lanes = slice(tile * LANES, (tile + 1) * LANES)
            at = base + tile * merge_share
            merge_out[source * merge_share : (source + 1) * merge_share, lanes] = all_s[
                source, at : at + merge_share
            ].astype(F32)
            at = base + 4 * merge_share + tile * head_share
            outw_out[source * head_share : (source + 1) * head_share, lanes] = all_s[
                source, at : at + head_share
            ].astype(F32)


def moved(block, axis, bits):
    count = lax.axis_size(axis)
    return lax.ppermute(block, axis, [(index, index ^ bits) for index in range(count)])


def over_streams(packs):
    return [packs[0]] + [moved(packs[bits], "stream", bits) for bits in range(1, lax.axis_size("stream"))]


def near_blocks(block):
    return [block] + [moved(block, "tm", bits) for bits in range(2, lax.axis_size("tm"), 2)]


def far_blocks(near):
    far = [moved(part, "tm", 1) for part in near]
    return [part for pair in zip(near, far) for part in pair]


def far_stack(near):
    stack = jnp.stack(near)
    return stack, moved(stack, "tm", 1)


def head_device(
    frames,
    lengths,
    cotangent,
    ln_attn_gain,
    ln_attn_bias,
    ln_mlp_gain,
    ln_mlp_bias,
    qkv_weight,
    content_bias,
    position_bias,
    pos_weight,
    out_weight,
    up_weight,
    up_bias,
    gate_norm_gain,
    gate_norm_bias,
    conv_kernel,
    conv_bias,
    down_weight,
    down_bias,
    merge_weight,
    merge_bias,
):
    count = lax.axis_size("tm")
    quarters = lax.axis_size("stream")
    own = frames.shape[1]
    total = own * count
    folded = total + total // 2
    padded = folded + 4 * MARGIN
    share = HALF // (quarters * count)
    channels = HALF // count
    quarter = D // quarters
    own_frames = frames[0]
    own_cotangent = cotangent[0]

    whole, late = Part(), Part(late=True)
    near = near_blocks(own_frames)
    cot_copies = jnp.broadcast_to(own_cotangent[None], (count, own, D))
    up_own, table, qkv_own, pos_own, bias_own = kernel_call(
        select_kernel,
        [
            ((D, 3 * LANES), BF16),
            ((2, 8 + KERNEL + 1, LANES), F32),
            ((D, 3 * LANES), BF16),
            ((D, LANES), BF16),
            ((8, LANES), F32),
        ],
        10 * "v",
    )(
        up_weight,
        up_bias,
        gate_norm_gain,
        gate_norm_bias,
        conv_bias,
        conv_kernel,
        qkv_weight,
        pos_weight,
        content_bias,
        position_bias,
    )
    frequency = jnp.exp(jnp.arange(D // 2, dtype=F32) * (-2.0 * math.log(10000.0) / D))
    coarse = jnp.arange(0, total, BLOCK, dtype=F32)[:, None] * frequency[None]
    fine = jnp.arange(BLOCK, dtype=F32)[:, None] * frequency[None]
    coarse_table = jnp.concatenate([jnp.sin(coarse), jnp.cos(coarse)], axis=1)
    fine_table = jnp.concatenate([jnp.sin(fine), jnp.cos(fine)], axis=1)
    near, up_own, coarse_table, fine_table, cot_copies = lax.optimization_barrier(
        (near, up_own, coarse_table, fine_table, cot_copies)
    )
    blocks = far_blocks(near)
    cot = lax.all_to_all(cot_copies, "tm", 0, 0, tiled=True).reshape(total, D)

    n_attn, n_mlp, hat, q_position, query, key, value, prob, attn, mean, rate = kernel_call(
        attend_kernel,
        [
            ((total, D), BF16, 1),
            ((total, D), BF16, 1),
            ((total, D), BF16, 1),
            ((total, LANES), BF16, 1),
            ((total, LANES + D), BF16, 1),
            ((total, LANES + D), BF16, 1),
            ((total, LANES), BF16, 1),
            ((total, total), BF16, 1),
            ((total, LANES), F32, 1),
            ((total, LANES), F32, 1),
            ((total, LANES), F32, 1),
        ],
        [
            "s",
            blocks_part(),
            *"vvvvvvvvv",
            Part((D, HALF), lambda refs, buffer: [(refs[0].at[:, pl.ds(HALF, HALF)], buffer)], late=True),
            "v",
        ],
        bounds=True,
    )(
        lengths,
        *blocks,
        ln_attn_gain,
        ln_attn_bias,
        ln_mlp_gain,
        ln_mlp_bias,
        qkv_own,
        pos_own,
        bias_own,
        coarse_table,
        fine_table,
        up_weight,
        up_bias,
    )

    def own_down(refs, buffer):
        place = lax.axis_index("tm")
        stride = HALF // quarters
        return [
            (
                refs[0].at[pl.ds(pl.multiple_of(part * stride + share * place, 16), share)],
                buffer.at[pl.ds(part * share, share)],
            )
            for part in range(quarters)
        ]

    mixed, gate_pre, grad_y, slope, gate_hat, early_pack, vectors, first_lines = kernel_call(
        mlp_first_kernel,
        [
            ((count, own + 16, 2 * LANES), BF16, 1),
            ((folded, LANES), BF16, 1),
            ((folded, LANES), BF16, 1),
            ((folded, LANES), BF16, 1),
            ((folded, LANES), BF16, 1),
            ((quarters, 8 * share, LANES), BF16, 1),
            ((channels, LANES), F32),
            ((8, D), F32),
        ],
        [
            "s",
            whole,
            "v",
            "v",
            whole,
            whole,
            late,
            rows_part(D, D, late=True),
            Part((2 * LANES, D), own_down, late=True),
            Part(late=True),
        ],
        [
            ((folded, LANES), F32),
            ((folded, LANES), F32),
            ((total, 2 * LANES), BF16),
            ((folded, LANES), F32),
            ((folded, LANES), F32),
            ((padded, LANES), F32),
            ((padded, LANES), F32),
            ((folded, LANES), F32),
            ((folded, LANES), F32),
            ((total, D), BF16),
            ((total, 2 * LANES), BF16),
            ((2, 32, 8, LANES), F32),
            ((2, 32, 8, LANES), F32),
            ((2, 32, 8, LANES), F32),
            ((total, LANES), F32),
            ((3, WINDOW + 2 * MARGIN, LANES), F32),
            ((3, WINDOW + 2 * MARGIN, LANES), F32),
        ],
        bounds=True,
    )(lengths, n_mlp, up_own, table, mean, rate, cot, merge_weight, down_weight, attn)
    mixed_own = lax.all_to_all(mixed, "tm", 0, 0, tiled=True)

    def own_head(refs, buffer):
        at = pl.ds(pl.multiple_of(lax.axis_index("tm") * HEAD, HEAD), HEAD)
        return [(refs[0].at[at], buffer.at[pl.ds(0, HEAD)])]

    branch, from_attn, *head_packs, head_lines = kernel_call(
        attend_back_kernel,
        [
            ((total, D), BF16, 1),
            ((total, D), BF16, 1),
            *([((4 * HEAD + 8 * share, LANES), BF16, 1)] * quarters),
            ((8, D), F32),
        ],
        [
            whole,
            rows_part(0, D),
            Part((LANES, D), own_head),
            whole,
            late,
            late,
            late,
            "v",
            "v",
            late,
            Part((total, LANES), lambda refs, buffer: [(refs[0].at[:, pl.ds(0, LANES)], buffer)], late=True),
            late,
            late,
            late,
            late,
            "v",
            late,
        ],
        [
            ((total, LANES), BF16),
            ((total, total), BF16),
            ((total, D), BF16),
            ((total, 3 * LANES), BF16),
            ((4 * HEAD, D), F32),
        ],
    )(
        cot,
        merge_weight,
        out_weight,
        attn,
        value,
        prob,
        key,
        coarse_table,
        fine_table,
        pos_own,
        query,
        n_attn,
        q_position,
        qkv_own,
        hat,
        ln_attn_gain,
        early_pack,
    )
    head_parts = over_streams(head_packs)
    mixed_own, _ = lax.optimization_barrier((mixed_own, head_lines))
    out_rows, joined = kernel_call(
        output_kernel,
        [((own, D), BF16), ((count, 256, own), BF16)],
        "vvvvvvv",
        megas=24,
    )(own_frames, mixed_own, out_weight, down_weight, down_bias, merge_weight, merge_bias)
    joined_all = lax.all_to_all(joined, "tm", 0, 0, tiled=True)
    gate_pre, _ = lax.optimization_barrier((gate_pre, joined))
    late_rows = 5 * share + 16 + 3 * D // count
    pre, same, apart, own_lines, up_columns = kernel_call(
        mlp_second_kernel,
        [
            ((total, 3 * LANES), BF16, 1),
            ((count // 2, own, D), BF16, 1),
            ((count // 2, own, D), BF16, 1),
            ((8, D), F32),
            ((channels, LANES), F32),
        ],
        [
            Part(
                (count, 2 * total // BLOCK, 2 * LANES),
                lambda refs, buffer: [(refs[0].at[:, pl.ds(own, 2 * total // BLOCK)], buffer)],
            ),
            *([whole] * 4),
            late,
            late,
            "v",
            late,
        ],
        [((total, 2 * LANES), F32)],
    )(mixed_own, gate_pre, grad_y, slope, gate_hat, up_own, hat, ln_mlp_gain, from_attn)
    sibling = moved(apart, "tm", 1)
    pre, joined_all = lax.optimization_barrier((pre, joined_all))
    (late_pack,) = kernel_call(
        late_pack_kernel,
        [((quarters, late_rows, LANES), BF16, 1)],
        [
            Part(
                (total, 2 * LANES),
                lambda refs, buffer: [(refs[0].at[:, pl.ds(LANES, 2 * LANES)], buffer)],
            ),
            whole,
            whole,
            whole,
            whole,
            *"vvvvv",
        ],
    )(pre, n_mlp, joined_all, branch, cot, vectors, up_columns, first_lines, head_lines, own_lines)
    late_pack, head_parts = lax.optimization_barrier((late_pack, head_parts))
    late_moved = lax.all_to_all(late_pack, "stream", 0, 0, tiled=True)
    (early_part,) = kernel_call(add_kernel, [((4 * HEAD + 8 * share, LANES), BF16)], quarters * "v", megas=24)(
        *head_parts
    )
    early_near = near_blocks(early_part)
    pairs = kernel_call(pair_kernel, [((own, D), BF16)] * (count // 2), "vv", megas=24)(same, sibling)
    late_moved, early_near, pairs = lax.optimization_barrier((late_moved, early_near, pairs))
    sums = [pairs[0]] + [moved(pairs[slot], "tm", 2 * slot) for slot in range(1, count // 2)]
    (late_part,) = kernel_call(add_streams_kernel, [((late_rows, LANES), BF16)], "v", megas=24)(late_moved)
    late_near = near_blocks(late_part)
    early_all = far_stack(early_near)
    grad_qkv, grad_pos, grad_down, half_up = kernel_call(
        early_kernel,
        [
            ((quarter, 3 * D), F32),
            ((quarter, D), F32),
            ((HALF // quarters, D), F32),
            ((quarter, 2 * HALF), F32, 1, (quarter, HALF), lambda ref: ref.at[:, pl.ds(0, HALF)]),
        ],
        "vv",
        [((count, 4 * HEAD + 8 * share, LANES), BF16)],
        megas=24,
    )(*early_all)
    late_near, grad_pos, sums = lax.optimization_barrier((late_near, grad_pos, sums))
    late_parts = far_stack(late_near)
    (grad_frames,) = kernel_call(frames_kernel, [((own, D), F32)], (2 + count // 2) * "v", megas=24)(
        own_frames, own_cotangent, *sums
    )
    late_parts, grad_frames = lax.optimization_barrier((late_parts, grad_frames))
    late = kernel_call(
        late_kernel,
        [((quarter,), F32)] * 6
        + [
            ((quarter, D), F32),
            ((quarter, 2 * HALF), F32, 1, (quarter, HALF), lambda ref: ref.at[:, pl.ds(HALF, HALF)]),
            ((2 * HALF // quarters,), F32),
            ((HALF // quarters,), F32),
            ((HALF // quarters,), F32),
            ((KERNEL, HALF // quarters), F32),
            ((HALF // quarters,), F32),
            ((quarter,), F32),
            ((2 * D // quarters, D), F32),
            ((quarter,), F32),
        ],
        "kvv",
        [((count,) + late_part.shape, BF16)],
        megas=24,
        aliases={0: 7},
    )(half_up, *late_parts)
    return (
        out_rows[None],
        grad_frames[None],
        *late[:4],
        grad_qkv,
        *late[4:6],
        grad_pos,
        *late[6:13],
        grad_down,
        *late[13:],
    )


def per_device(*operands):
    fits = (
        lax.axis_size("tm") == HEADS
        and lax.axis_size("stream") * LANES == D
        and operands[0].shape[1] == BLOCK
    )
    return head_device(*operands) if fits else frame_device(*operands)


def solution(mesh):
    return jax.shard_map(
        per_device,
        mesh=mesh,
        in_specs=(
            P("stream", "tm", None),
            P("stream", None),
            P("stream", "tm", None),
            P(),
            P(),
            P(),
            P(),
            P(),
            P(),
            P(),
            P(),
            P(),
            P(),
            P(),
            P(),
            P(),
            P(),
            P(),
            P(),
            P(),
            P(),
            P(),
        ),
        out_specs=(
            P("stream", "tm", None),
            P("stream", "tm", None),
            P("stream"),
            P("stream"),
            P("stream"),
            P("stream"),
            P("stream", None),
            P("stream"),
            P("stream"),
            P("stream", None),
            P("stream", None),
            P("stream", None),
            P("stream"),
            P("stream"),
            P("stream"),
            P(None, "stream"),
            P("stream"),
            P("stream", None),
            P("stream"),
            P("stream", None),
            P("stream"),
        ),
        check_vma=False,
    )
```

```python
import math

import jax
import jax.numpy as jnp
from jax import lax
from jax.experimental import pallas as pl
from jax.experimental.pallas import tpu as pltpu
from jax.sharding import PartitionSpec as P

D = 512
HEADS = 8
HEAD = 64
KERNEL = 31
ITEMS = 5
HALF = 1536


EPS = 1e-05
MASKED = -1e30


def extended(block, sides, width):
    for axis, dim in sides:
        count = lax.axis_size(axis)
        forward = [(i, i + 1) for i in range(count - 1)]
        backward = [(target, source) for source, target in forward]
        low = lax.ppermute(
            lax.slice_in_dim(block, block.shape[dim] - width, None, axis=dim), axis, forward
        )
        high = lax.ppermute(lax.slice_in_dim(block, 0, width, axis=dim), axis, backward)
        block = jnp.concatenate([low, block, high], axis=dim)
    return block


def norm_rows(inputs, scale_row, shift_row):
    row_mean = jnp.mean(inputs, axis=-1, keepdims=True)
    centred = inputs - row_mean
    spread = jnp.mean(centred * centred, axis=-1, keepdims=True)
    return centred * lax.rsqrt(spread + EPS) * scale_row + shift_row


def gelu_exact(inputs):
    return jax.nn.gelu(inputs, approximate=False)


def frame_info(lengths, offset, extent):
    item_ends = jnp.cumsum(lengths)
    first_table = jnp.concatenate([item_ends - lengths, item_ends[-1:]])
    frame_index = offset + jnp.arange(extent, dtype=jnp.int32)
    item_of = jnp.sum((frame_index[:, None] >= item_ends[None, :]).astype(jnp.int32), axis=1)
    labels = jnp.arange(ITEMS + 1, dtype=jnp.int32)
    first_frame = jnp.sum(
        jnp.where(item_of[:, None] == labels[None, :], first_table[None, :], 0), axis=1
    )
    return (frame_index, item_of, frame_index - first_frame)


def angles(place_in):
    frequency = jnp.exp(jnp.arange(D // 2, dtype=jnp.float32) * (-2.0 * math.log(10000.0) / D))
    phase_angle = place_in.astype(jnp.float32)[:, None] * frequency[None, :]
    return (jnp.sin(phase_angle), jnp.cos(phase_angle))


def rel_query(projected, sine_rows, cosine_rows):
    half_size = projected.shape[-1] // 2
    first_half = projected[..., :half_size]
    second_half = projected[..., half_size:]
    sine_wide = sine_rows[:, None, :]
    cosine_wide = cosine_rows[:, None, :]
    return jnp.concatenate(
        [
            first_half * sine_wide + second_half * cosine_wide,
            second_half * sine_wide - first_half * cosine_wide,
        ],
        axis=-1,
    )


def step_size(extent):
    return math.gcd(extent, 512)


def score_block(q_content, q_rel, query_item, query_frame, key_block, key_start, lengths):
    extent = key_block.shape[0]
    key_frame, key_item, key_place = frame_info(lengths, key_start, extent)
    sine_rows, cosine_rows = angles(key_place)
    k_rel = jnp.concatenate([cosine_rows, sine_rows], axis=1).astype(jnp.bfloat16)
    raw_scores = jnp.einsum(
        "qhe,khe->hqk",
        q_content,
        key_block.reshape(extent, HEADS, HEAD),
        preferred_element_type=jnp.float32,
    )
    raw_scores = raw_scores + jnp.einsum(
        "qhc,kc->hqk", q_rel, k_rel, preferred_element_type=jnp.float32
    )
    allowed = (query_item[:, None] == key_item[None, :]) & (
        (query_item[:, None] < ITEMS) | (query_frame[:, None] == key_frame[None, :])
    )
    return (raw_scores, allowed, k_rel)


def block_grads(
    q_content,
    q_rel,
    query_item,
    query_frame,
    grad_out,
    log_total,
    delta_rows,
    key_block,
    value_block,
    key_start,
    lengths,
):
    extent = key_block.shape[0]
    raw_scores, allowed, k_rel = score_block(
        q_content, q_rel, query_item, query_frame, key_block, key_start, lengths
    )
    prob_rows = jnp.where(allowed[None], jnp.exp(raw_scores * 0.125 - log_total[:, :, None]), 0.0)
    grad_prob = jnp.einsum(
        "qhe,khe->hqk",
        grad_out,
        value_block.reshape(extent, HEADS, HEAD),
        preferred_element_type=jnp.float32,
    )
    grad_raw = (prob_rows * (grad_prob - delta_rows[:, :, None]) * 0.125).astype(jnp.bfloat16)
    return (prob_rows.astype(jnp.bfloat16), grad_raw, k_rel)


def frame_device(
    frames,
    lengths,
    cotangent,
    ln_attn_gain,
    ln_attn_bias,
    ln_mlp_gain,
    ln_mlp_bias,
    qkv_weight,
    content_bias,
    position_bias,
    pos_weight,
    out_weight,
    up_weight,
    up_bias,
    gate_norm_gain,
    gate_norm_bias,
    conv_kernel,
    conv_bias,
    down_weight,
    down_bias,
    merge_weight,
    merge_bias,
):
    row_count = frames.shape[1]
    cycle_size = lax.axis_size("tm")
    offset = lax.axis_index("tm") * row_count
    stream_lengths = lengths[0]
    inputs = frames[0].astype(jnp.float32)
    frame_index, item_of, place_in = frame_info(stream_lengths, offset, row_count)
    sine_rows, cosine_rows = angles(place_in)
    attn_norm, attn_pull = jax.vjp(
        norm_rows, inputs, ln_attn_gain.astype(jnp.float32), ln_attn_bias.astype(jnp.float32)
    )
    mlp_norm, mlp_pull = jax.vjp(
        norm_rows, inputs, ln_mlp_gain.astype(jnp.float32), ln_mlp_bias.astype(jnp.float32)
    )
    attn_norm_low = attn_norm.astype(jnp.bfloat16)
    mlp_norm_low = mlp_norm.astype(jnp.bfloat16)
    qkv_rows = jnp.dot(attn_norm_low, qkv_weight, preferred_element_type=jnp.float32)
    query_rows = qkv_rows[:, :D]
    key_rows = qkv_rows[:, D : 2 * D].astype(jnp.bfloat16)
    value_rows = qkv_rows[:, 2 * D :].astype(jnp.bfloat16)
    q_content = (query_rows + content_bias.astype(jnp.float32)).astype(jnp.bfloat16)
    q_position = (query_rows + position_bias.astype(jnp.float32)).astype(jnp.bfloat16)
    content_heads = q_content.reshape(row_count, HEADS, HEAD)
    position_heads = q_position.reshape(row_count, HEADS, HEAD)
    pos_heads = pos_weight.reshape(D, HEADS, HEAD)
    projected = jnp.einsum(
        "the,che->thc", position_heads, pos_heads, preferred_element_type=jnp.float32
    )
    q_rel = rel_query(projected, sine_rows, cosine_rows).astype(jnp.bfloat16)
    start_state = (
        jnp.full((HEADS, row_count), MASKED, jnp.float32),
        jnp.zeros((HEADS, row_count), jnp.float32),
        jnp.zeros((HEADS, row_count, HEAD), jnp.float32),
    )
    fold_state = start_state
    key_piece = lax.all_gather(key_rows, "tm", axis=0, tiled=True)
    value_piece = lax.all_gather(value_rows, "tm", axis=0, tiled=True)
    extent = key_piece.shape[0]
    step_rows = step_size(extent)

    def forward_one_step(inner_state, step_index):
        row_top, row_total, row_acc = inner_state
        key_block = lax.dynamic_slice_in_dim(key_piece, step_index * step_rows, step_rows, 0)
        value_block = lax.dynamic_slice_in_dim(value_piece, step_index * step_rows, step_rows, 0)
        raw_scores, allowed, k_rel = score_block(
            content_heads,
            q_rel,
            item_of,
            frame_index,
            key_block,
            step_index * step_rows,
            stream_lengths,
        )
        scaled = jnp.where(allowed[None], raw_scores * 0.125, MASKED)
        new_top = jnp.maximum(row_top, jnp.max(scaled, axis=2))
        weight = jnp.where(allowed[None], jnp.exp(scaled - new_top[:, :, None]), 0.0)
        factor = jnp.exp(row_top - new_top)
        row_total = row_total * factor + jnp.sum(weight, axis=2)
        row_acc = row_acc * factor[:, :, None] + jnp.einsum(
            "hqk,khe->hqe",
            weight.astype(jnp.bfloat16),
            value_block.reshape(step_rows, HEADS, HEAD),
            preferred_element_type=jnp.float32,
        )
        return ((new_top, row_total, row_acc), None)

    fold_state, unused = lax.scan(
        forward_one_step, fold_state, jnp.arange(extent // step_rows, dtype=jnp.int32)
    )
    row_top, row_total, row_acc = fold_state
    attn_heads = row_acc / row_total[:, :, None]
    log_total = row_top + jnp.log(row_total)
    attn_low = jnp.transpose(attn_heads, (1, 0, 2)).reshape(row_count, D).astype(jnp.bfloat16)
    branch_attn = jnp.dot(attn_low, out_weight, preferred_element_type=jnp.float32).astype(
        jnp.bfloat16
    )
    hidden_pre = jnp.dot(
        mlp_norm_low, up_weight, preferred_element_type=jnp.float32
    ) + up_bias.astype(jnp.float32)
    hidden, gelu_pull = jax.vjp(gelu_exact, hidden_pre)
    gate_half = hidden[:, :HALF]
    conv_norm, conv_pull = jax.vjp(
        norm_rows,
        hidden[:, HALF:],
        gate_norm_gain.astype(jnp.float32),
        gate_norm_bias.astype(jnp.float32),
    )
    conv_in = conv_norm.astype(jnp.bfloat16)
    half_width = KERNEL // 2
    conv_wide = extended(conv_in, (("tm", 0),), half_width)
    wide_frame, wide_item, wide_place = frame_info(
        stream_lengths, offset - half_width, row_count + 2 * half_width
    )
    kernel_rows = conv_kernel.astype(jnp.float32)
    conv_out = conv_bias.astype(jnp.float32) + jnp.zeros_like(gate_half)
    for tap_index in range(KERNEL):
        same_item = (wide_item[tap_index : tap_index + row_count] == item_of)[:, None]
        conv_out = (
            conv_out
            + jnp.where(
                same_item, conv_wide[tap_index : tap_index + row_count].astype(jnp.float32), 0.0
            )
            * kernel_rows[tap_index]
        )
    gated_low = (gate_half * conv_out).astype(jnp.bfloat16)
    branch_mlp = (
        jnp.dot(gated_low, down_weight, preferred_element_type=jnp.float32)
        + down_bias.astype(jnp.float32)
    ).astype(jnp.bfloat16)
    joined = jnp.concatenate([branch_attn, branch_mlp], axis=1)
    result = (
        inputs
        + jnp.dot(joined, merge_weight, preferred_element_type=jnp.float32)
        + merge_bias.astype(jnp.float32)
    )
    out_rows = result.astype(jnp.bfloat16)[None]
    grad_low = cotangent[0]
    grad_rows = grad_low.astype(jnp.float32)
    grad_merge_bias = jnp.sum(grad_rows, axis=0)
    grad_merge_weight = jnp.einsum(
        "tc,td->cd", joined, grad_low, preferred_element_type=jnp.float32
    )
    grad_joined = jnp.einsum(
        "td,cd->tc", grad_low, merge_weight, preferred_element_type=jnp.float32
    )
    grad_attn_branch = grad_joined[:, :D].astype(jnp.bfloat16)
    grad_mlp_branch = grad_joined[:, D:].astype(jnp.bfloat16)
    grad_down_weight = jnp.einsum(
        "tc,td->cd", gated_low, grad_mlp_branch, preferred_element_type=jnp.float32
    )
    grad_down_bias = jnp.sum(grad_mlp_branch.astype(jnp.float32), axis=0)
    grad_gated = jnp.einsum(
        "td,cd->tc", grad_mlp_branch, down_weight, preferred_element_type=jnp.float32
    )
    grad_gate_half = grad_gated * conv_out
    grad_conv_out = (grad_gated * gate_half).astype(jnp.bfloat16)
    grad_conv_rows = grad_conv_out.astype(jnp.float32)
    grad_conv_bias = jnp.sum(grad_conv_rows, axis=0)
    grad_wide = extended(grad_conv_out, (("tm", 0),), half_width)
    kernel_list = []
    grad_conv_in = jnp.zeros_like(grad_conv_rows)
    for tap_index in range(KERNEL):
        same_item = (wide_item[tap_index : tap_index + row_count] == item_of)[:, None]
        kernel_list.append(
            jnp.sum(
                jnp.where(
                    same_item, conv_wide[tap_index : tap_index + row_count].astype(jnp.float32), 0.0
                )
                * grad_conv_rows,
                axis=0,
            )
        )
        back_start = 2 * half_width - tap_index
        back_item = (wide_item[back_start : back_start + row_count] == item_of)[:, None]
        grad_conv_in = (
            grad_conv_in
            + jnp.where(
                back_item, grad_wide[back_start : back_start + row_count].astype(jnp.float32), 0.0
            )
            * kernel_rows[tap_index]
        )
    grad_conv_kernel = jnp.stack(kernel_list)
    grad_second, grad_gate_norm_gain, grad_gate_norm_bias = conv_pull(grad_conv_in)
    (grad_pre_rows,) = gelu_pull(jnp.concatenate([grad_gate_half, grad_second], axis=1))
    grad_pre = grad_pre_rows.astype(jnp.bfloat16)
    grad_up_bias = jnp.sum(grad_pre.astype(jnp.float32), axis=0)
    grad_up_weight = jnp.einsum(
        "tc,tf->cf", mlp_norm_low, grad_pre, preferred_element_type=jnp.float32
    )
    grad_mlp_norm = jnp.einsum("tf,cf->tc", grad_pre, up_weight, preferred_element_type=jnp.float32)
    grad_out_weight = jnp.einsum(
        "tc,td->cd", attn_low, grad_attn_branch, preferred_element_type=jnp.float32
    )
    grad_attn_low = jnp.einsum(
        "td,cd->tc", grad_attn_branch, out_weight, preferred_element_type=jnp.float32
    ).astype(jnp.bfloat16)
    grad_out_heads = grad_attn_low.reshape(row_count, HEADS, HEAD)
    delta_rows = jnp.sum(
        jnp.transpose(grad_out_heads.astype(jnp.float32), (1, 0, 2)) * attn_heads, axis=2
    )
    total_frames = row_count * cycle_size
    back_start_state = (
        jnp.zeros((row_count, HEADS, HEAD), jnp.float32),
        jnp.zeros((row_count, HEADS, D), jnp.float32),
        jnp.zeros((total_frames, D), jnp.float32),
        jnp.zeros((total_frames, D), jnp.float32),
    )
    back_key_piece = lax.all_gather(key_rows, "tm", axis=0, tiled=True)
    back_value_piece = lax.all_gather(value_rows, "tm", axis=0, tiled=True)
    extent = back_key_piece.shape[0]
    back_step_rows = step_size(extent)

    def back_one_step(inner_state, step_index):
        grad_content, grad_rel = inner_state
        key_block = lax.dynamic_slice_in_dim(
            back_key_piece, step_index * back_step_rows, back_step_rows, 0
        )
        value_block = lax.dynamic_slice_in_dim(
            back_value_piece, step_index * back_step_rows, back_step_rows, 0
        )
        prob_low, grad_raw, k_rel = block_grads(
            content_heads,
            q_rel,
            item_of,
            frame_index,
            grad_out_heads,
            log_total,
            delta_rows,
            key_block,
            value_block,
            step_index * back_step_rows,
            stream_lengths,
        )
        grad_content = grad_content + jnp.einsum(
            "hqk,khe->qhe",
            grad_raw,
            key_block.reshape(back_step_rows, HEADS, HEAD),
            preferred_element_type=jnp.float32,
        )
        grad_rel = grad_rel + jnp.einsum(
            "hqk,kc->qhc", grad_raw, k_rel, preferred_element_type=jnp.float32
        )
        key_part = jnp.einsum(
            "hqk,qhe->khe", grad_raw, content_heads, preferred_element_type=jnp.float32
        ).reshape(back_step_rows, D)
        value_part = jnp.einsum(
            "hqk,qhe->khe", prob_low, grad_out_heads, preferred_element_type=jnp.float32
        ).reshape(back_step_rows, D)
        return ((grad_content, grad_rel), (key_part, value_part))

    inner_state, block_parts = lax.scan(
        back_one_step,
        (back_start_state[0], back_start_state[1]),
        jnp.arange(extent // back_step_rows, dtype=jnp.int32),
    )
    key_all = block_parts[0].reshape(extent, D)
    value_all = block_parts[1].reshape(extent, D)
    grad_content, grad_rel, key_all, value_all = (
        inner_state[0],
        inner_state[1],
        key_all,
        value_all,
    )
    grad_keys, grad_values = (
        lax.psum_scatter(key_all, "tm", scatter_dimension=0, tiled=True),
        lax.psum_scatter(value_all, "tm", scatter_dimension=0, tiled=True),
    )
    half_size = D // 2
    rel_first = grad_rel[..., :half_size]
    rel_second = grad_rel[..., half_size:]
    sine_wide = sine_rows[:, None, :]
    cosine_wide = cosine_rows[:, None, :]
    grad_projected = jnp.concatenate(
        [
            rel_first * sine_wide - rel_second * cosine_wide,
            rel_first * cosine_wide + rel_second * sine_wide,
        ],
        axis=-1,
    ).astype(jnp.bfloat16)
    grad_pos_weight = jnp.einsum(
        "thc,the->che", grad_projected, position_heads, preferred_element_type=jnp.float32
    ).reshape(D, D)
    grad_q_position = jnp.einsum(
        "thc,che->the", grad_projected, pos_heads, preferred_element_type=jnp.float32
    )
    grad_content_bias = jnp.sum(grad_content, axis=0).reshape(D)
    grad_position_bias = jnp.sum(grad_q_position, axis=0).reshape(D)
    grad_query = (grad_content + grad_q_position).reshape(row_count, D).astype(jnp.bfloat16)
    grad_qkv = jnp.concatenate(
        [grad_query, grad_keys.astype(jnp.bfloat16), grad_values.astype(jnp.bfloat16)], axis=1
    )
    grad_qkv_weight = jnp.einsum(
        "tc,tf->cf", attn_norm_low, grad_qkv, preferred_element_type=jnp.float32
    )
    grad_attn_norm = jnp.einsum(
        "tf,cf->tc", grad_qkv, qkv_weight, preferred_element_type=jnp.float32
    )
    grad_from_attn, grad_ln_attn_gain, grad_ln_attn_bias = attn_pull(grad_attn_norm)
    grad_from_mlp, grad_ln_mlp_gain, grad_ln_mlp_bias = mlp_pull(grad_mlp_norm)
    grad_inputs = grad_rows + grad_from_attn + grad_from_mlp
    weight_grads = (
        grad_ln_attn_gain,
        grad_ln_attn_bias,
        grad_ln_mlp_gain,
        grad_ln_mlp_bias,
        grad_qkv_weight,
        grad_content_bias,
        grad_position_bias,
        grad_pos_weight,
        grad_out_weight,
        grad_up_weight,
        grad_up_bias,
        grad_gate_norm_gain,
        grad_gate_norm_bias,
        grad_conv_kernel,
        grad_conv_bias,
        grad_down_weight,
        grad_down_bias,
        grad_merge_weight,
        grad_merge_bias,
    )
    summed = lax.psum(
        (
            weight_grads[0],
            weight_grads[1],
            weight_grads[2],
            weight_grads[3],
            weight_grads[4],
            weight_grads[5],
            weight_grads[6],
            weight_grads[7],
            weight_grads[8],
            weight_grads[9],
            weight_grads[10],
            weight_grads[11],
            weight_grads[12],
            weight_grads[13],
            weight_grads[14],
            weight_grads[15],
            weight_grads[16],
            weight_grads[17],
            weight_grads[18],
        ),
        "tm",
    )
    shares = (
        lax.psum_scatter(
            summed[0].astype(jnp.bfloat16), "stream", scatter_dimension=0, tiled=True
        ).astype(jnp.float32),
        lax.psum_scatter(
            summed[1].astype(jnp.bfloat16), "stream", scatter_dimension=0, tiled=True
        ).astype(jnp.float32),
        lax.psum_scatter(
            summed[2].astype(jnp.bfloat16), "stream", scatter_dimension=0, tiled=True
        ).astype(jnp.float32),
        lax.psum_scatter(
            summed[3].astype(jnp.bfloat16), "stream", scatter_dimension=0, tiled=True
        ).astype(jnp.float32),
        lax.psum_scatter(
            summed[4].astype(jnp.bfloat16), "stream", scatter_dimension=0, tiled=True
        ).astype(jnp.float32),
        lax.psum_scatter(
            summed[5].astype(jnp.bfloat16), "stream", scatter_dimension=0, tiled=True
        ).astype(jnp.float32),
        lax.psum_scatter(
            summed[6].astype(jnp.bfloat16), "stream", scatter_dimension=0, tiled=True
        ).astype(jnp.float32),
        lax.psum_scatter(
            summed[7].astype(jnp.bfloat16), "stream", scatter_dimension=0, tiled=True
        ).astype(jnp.float32),
        lax.psum_scatter(
            summed[8].astype(jnp.bfloat16), "stream", scatter_dimension=0, tiled=True
        ).astype(jnp.float32),
        lax.psum_scatter(
            summed[9].astype(jnp.bfloat16), "stream", scatter_dimension=0, tiled=True
        ).astype(jnp.float32),
        lax.psum_scatter(
            summed[10].astype(jnp.bfloat16), "stream", scatter_dimension=0, tiled=True
        ).astype(jnp.float32),
        lax.psum_scatter(
            summed[11].astype(jnp.bfloat16), "stream", scatter_dimension=0, tiled=True
        ).astype(jnp.float32),
        lax.psum_scatter(
            summed[12].astype(jnp.bfloat16), "stream", scatter_dimension=0, tiled=True
        ).astype(jnp.float32),
        lax.psum_scatter(
            summed[13].astype(jnp.bfloat16), "stream", scatter_dimension=1, tiled=True
        ).astype(jnp.float32),
        lax.psum_scatter(
            summed[14].astype(jnp.bfloat16), "stream", scatter_dimension=0, tiled=True
        ).astype(jnp.float32),
        lax.psum_scatter(
            summed[15].astype(jnp.bfloat16), "stream", scatter_dimension=0, tiled=True
        ).astype(jnp.float32),
        lax.psum_scatter(
            summed[16].astype(jnp.bfloat16), "stream", scatter_dimension=0, tiled=True
        ).astype(jnp.float32),
        lax.psum_scatter(
            summed[17].astype(jnp.bfloat16), "stream", scatter_dimension=0, tiled=True
        ).astype(jnp.float32),
        lax.psum_scatter(
            summed[18].astype(jnp.bfloat16), "stream", scatter_dimension=0, tiled=True
        ).astype(jnp.float32),
    )
    return (out_rows, grad_inputs[None]) + tuple(shares)


LANES = 128
LOW = LANES // 2
BLOCK = 128
TALL = 256
WINDOW = 64
MARGIN = 16
BOUNDS = 16
MEGA = 1024 * 1024
F32 = jnp.float32
BF16 = jnp.bfloat16


def dot_nn(left, right):
    return jnp.dot(left, right, preferred_element_type=F32)


def dot_nt(left, right):
    return lax.dot_general(left, right, (((1,), (1,)), ((), ())), preferred_element_type=F32)


def dot_tn(left, right):
    return lax.dot_general(left, right, (((0,), (0,)), ((), ())), preferred_element_type=F32)


def rows_of(index, size, base=0):
    return pl.ds(pl.multiple_of(index * size, size) + base, size)


def line_of(ref):
    return ref[...].astype(F32).reshape(1, ref.shape[0])


def fold_rows(values):
    return jnp.sum(values.reshape(values.shape[0] // 8, 8, values.shape[1]), axis=0)


def one_row(values):
    return jnp.sum(values, axis=0, keepdims=True)


def turn(values):
    return pltpu.roll(values, LOW, 1)


def low_lanes(rows):
    return lax.broadcasted_iota(jnp.int32, (rows, LANES), 1) < LOW


def centre_rows(inputs):
    mean = jnp.mean(inputs, axis=-1, keepdims=True)
    centred = inputs - mean
    spread = jnp.mean(centred * centred, axis=-1, keepdims=True)
    return centred * lax.rsqrt(spread + EPS)


def gelu_parts(values):
    phi = 0.5 + 0.5 * lax.erf(values * math.sqrt(0.5))
    bell = jnp.exp(values * values * -0.5)
    return values * phi, phi + values * bell * (1.0 / math.sqrt(2.0 * math.pi))


class Part:
    def __init__(self, shape=None, pairs=None, refs=1, late=False):
        self.shape, self.pairs, self.refs, self.late = shape, pairs, refs, late

    def buffer(self, operand):
        return self.shape or operand.shape

    def copies(self, refs, buffer):
        return self.pairs(refs, buffer) if self.pairs else [(refs[0], buffer)]


def blocks_part(half, late=False):
    def pairs(refs, buffer):
        place = lax.axis_index("tm")
        return [
            (
                ref.at[:, pl.ds(half * D, D)],
                buffer.at[rows_of(lax.bitwise_xor(jnp.int32(apart), place), BLOCK)],
            )
            for apart, ref in enumerate(refs)
        ]

    return Part((HEADS * BLOCK, D), pairs, HEADS, late)


def rows_part(first, size, late=False):
    return Part((size, D), lambda refs, buffer: [(refs[0].at[pl.ds(first, size)], buffer)], late=late)


class Fetch:
    def __init__(self, pairs, buffer, sems, first):
        self.buffer, self.begun = buffer, False
        self.pending = [
            pltpu.make_async_copy(source, target, sems.at[first + index])
            for index, (source, target) in enumerate(pairs)
        ]

    def begin(self):
        if not self.begun:
            for copy in self.pending:
                copy.start()
        self.begun = True

    def __call__(self):
        self.begin()
        for copy in self.pending:
            copy.wait()
        self.pending = []
        return self.buffer


def begin(*fetches):
    for fetch in fetches:
        fetch.begin()


class Send:
    def __init__(self, buffer, target, sems):
        self.buffer, self.target, self.sems, self.copies = buffer, target, sems, []

    def go(self, *index):
        source, target = (self.buffer.at[index], self.target.at[index]) if index else (self.buffer, self.target)
        copy = pltpu.make_async_copy(source, target, self.sems[len(self.copies)])
        copy.start()
        self.copies.append(copy)

    def finish(self):
        if not self.copies:
            self.go()


SPACES = {"v": pltpu.VMEM, "s": pltpu.SMEM, "k": pl.ANY}


def kernel_call(body, out_shapes, plan, scratch=(), megas=58, bounds=False, aliases=None):
    def call(*operands):
        in_specs, buffers, at = [], [], 0
        for item in plan:
            if item == "f":
                in_specs.append(pl.BlockSpec(memory_space=pl.ANY))
                buffers.append(pltpu.VMEM(operands[at].shape, operands[at].dtype))
                at += 1
            elif isinstance(item, Part):
                in_specs += [pl.BlockSpec(memory_space=pl.ANY)] * item.refs
                buffers.append(pltpu.VMEM(item.buffer(operands[at]), operands[at].dtype))
                at += item.refs
            else:
                in_specs.append(pl.BlockSpec(memory_space=SPACES[item]))
                at += 1
        sent = [out for out in out_shapes if len(out) > 2]
        buffers += [pltpu.VMEM(out[3] if len(out) > 3 else out[0], out[1]) for out in sent]
        sem_count = 96
        extra = [pltpu.SMEM((BOUNDS,), jnp.int32)] if bounds else []

        def outer(*refs):
            inputs, rest = refs[: len(in_specs)], refs[len(in_specs) :]
            outputs, rest = rest[: len(out_shapes)], rest[len(out_shapes) :]
            held, rest = list(rest[: len(buffers)]), rest[len(buffers) :]
            sems, rest = rest[0], rest[1:]
            given, at, used = [], 0, 0
            for item in plan:
                if item == "f":
                    given.append(Fetch([(inputs[at], held[0])], held.pop(0), sems, used))
                    given[-1].begin()
                    used += 1
                    at += 1
                elif isinstance(item, Part):
                    buffer = held.pop(0)
                    pairs = item.copies(inputs[at : at + item.refs], buffer)
                    given.append(Fetch(pairs, buffer, sems, used))
                    if not item.late:
                        given[-1].begin()
                    used += len(pairs)
                    at += item.refs
                else:
                    given.append(inputs[at])
                    at += 1
            results = []
            for out, ref in zip(out_shapes, outputs):
                if len(out) > 2:
                    target = out[4](ref) if len(out) > 3 else ref
                    results.append(Send(held.pop(0), target, [sems.at[used + index] for index in range(4)]))
                    used += 4
                else:
                    results.append(ref)
            assert used <= sem_count
            given = [item() if kind == "f" else item for kind, item in zip(plan, given)]
            body(*given, *results, *rest)
            for item in given:
                if isinstance(item, Fetch):
                    item()
            sends = [item for item in results if isinstance(item, Send)]
            for item in sends:
                item.finish()
            for item in sends:
                for copy in item.copies:
                    copy.wait()

        return pl.pallas_call(
            outer,
            out_shape=[jax.ShapeDtypeStruct(out[0], out[1]) for out in out_shapes],
            in_specs=in_specs,
            out_specs=[pl.BlockSpec(memory_space=pl.ANY if len(out) > 2 else pltpu.VMEM) for out in out_shapes],
            scratch_shapes=buffers
            + [pltpu.SemaphoreType.DMA((sem_count,))]
            + [pltpu.VMEM(shape, kind) for shape, kind in scratch]
            + extra,
            input_output_aliases=aliases or {},
            compiler_params=pltpu.CompilerParams(vmem_limit_bytes=megas * MEGA),
            cost_estimate=pl.CostEstimate(flops=0, bytes_accessed=0, transcendentals=0),
        )(*operands)

    return call


def fill_bounds(lengths_ref, bounds_s, total):
    bounds_s[0] = jnp.int32(0)
    end = jnp.int32(0)
    for item in range(ITEMS):
        end = end + lengths_ref[0, item]
        bounds_s[item + 1] = end
    for item in range(ITEMS + 1, BOUNDS):
        bounds_s[item] = jnp.int32(total)


def select_kernel(
    up_ref,
    up_bias_ref,
    gain_ref,
    bias_ref,
    conv_bias_ref,
    taps_ref,
    qkv_ref,
    pos_ref,
    content_ref,
    position_ref,
    up_out,
    table_out,
    qkv_out,
    pos_out,
    bias_out,
):
    place = lax.axis_index("tm")
    quarters = lax.axis_size("stream")
    share = HALF // (quarters * lax.axis_size("tm"))
    lane = lax.broadcasted_iota(jnp.int32, (1, 2 * LANES), 1)
    channel = jnp.where(lane < LANES + LOW, lane, lane - LOW)
    group = jnp.zeros_like(channel)
    for quarter in range(1, quarters):
        group = group + (channel >= quarter * share).astype(jnp.int32)
    source = group * (HALF // quarters) + share * place + channel - group * share
    chosen = (lax.broadcasted_iota(jnp.int32, (HALF, 2 * LANES), 0) == source).astype(F32).astype(BF16)
    gate = dot_nn(up_ref[:, :HALF], chosen)
    conv = dot_nn(up_ref[:, HALF:], chosen)
    up_out[:, :LANES] = gate[:, :LANES].astype(BF16)
    up_out[:, LANES : 2 * LANES] = jnp.where(low_lanes(D), gate[:, LANES:], conv[:, LANES:]).astype(BF16)
    up_out[:, 2 * LANES :] = conv[:, :LANES].astype(BF16)
    up_bias = line_of(up_bias_ref)
    lines = jnp.concatenate(
        [
            up_bias[:, :HALF],
            up_bias[:, HALF:],
            line_of(gain_ref),
            line_of(bias_ref),
            line_of(conv_bias_ref),
            jnp.zeros((3, HALF), F32),
        ],
        axis=0,
    )
    lines = dot_nn(lines.astype(BF16), chosen)
    taps = dot_nn(taps_ref[...], chosen)
    for part in range(2):
        lanes = slice(part * LANES, (part + 1) * LANES)
        table_out[part, :8] = lines[:, lanes]
        table_out[part, 8 : 8 + KERNEL] = taps[:, lanes]
        table_out[part, 8 + KERNEL :] = jnp.zeros((1, LANES), F32)

    odd = lax.rem(place, 2) == 1

    def head_lanes(ref, base):
        at = pl.ds(pl.multiple_of(lax.div(place, 2) * LANES + base, LANES), LANES)
        values = ref[:, at].astype(F32)
        values = jnp.where(odd, turn(values), values)
        return jnp.where(low_lanes(values.shape[0]), values, 0.0)

    for part in range(3):
        qkv_out[:, part * LANES : (part + 1) * LANES] = head_lanes(qkv_ref, part * D).astype(BF16)
    pos_out[...] = head_lanes(pos_ref, 0).astype(BF16)
    bias_out[...] = jnp.zeros((8, LANES), F32)
    for line, ref in enumerate((content_ref, position_ref)):
        values = line_of(ref)
        picked = values[:, :LANES]
        for tile in range(1, D // LANES):
            picked = jnp.where(
                lax.div(place, 2) == tile, values[:, tile * LANES : (tile + 1) * LANES], picked
            )
        picked = jnp.where(odd, turn(picked), picked)
        bias_out[line : line + 1] = jnp.where(low_lanes(1), picked, 0.0)


def angle_rows(coarse_ref, fine_ref, block, rows):
    half = D // 2
    base = coarse_ref[pl.ds(block, 1)]
    base_sine, base_cosine = base[:, :half], base[:, half:]
    sine, cosine = fine_ref[rows, :half], fine_ref[rows, half:]
    return base_sine * cosine + base_cosine * sine, base_cosine * cosine - base_sine * sine


def item_codes(bounds_s, index):
    code = jnp.zeros_like(index)
    for item in range(1, ITEMS + 1):
        code = code + (index >= bounds_s[item]).astype(jnp.int32)
    return jnp.where(code < ITEMS, code, ITEMS + index)


def attend_kernel(
    lengths_ref,
    x_ref,
    attn_gain_ref,
    attn_bias_ref,
    mlp_gain_ref,
    mlp_bias_ref,
    qkv_ref,
    pos_ref,
    bias_ref,
    coarse_ref,
    fine_ref,
    up_ref,
    up_bias_ref,
    n_attn_out,
    n_mlp_out,
    hat_out,
    q_position_out,
    query_out,
    key_out,
    value_out,
    prob_out,
    attn_out,
    mean_out,
    rate_out,
    bounds_s,
):
    frames = n_attn_out.buffer.shape[0]
    half = D // 2
    fill_bounds(lengths_ref, bounds_s, frames)
    attn_gain, attn_bias = line_of(attn_gain_ref), line_of(attn_bias_ref)
    mlp_gain, mlp_bias = line_of(mlp_gain_ref), line_of(mlp_bias_ref)
    content, position = bias_ref[0:1], bias_ref[1:2]
    x_ref = x_ref()
    begin(up_ref)
    lane = lax.broadcasted_iota(jnp.int32, (1, LANES), 1)
    spare = ((lane == HEAD) | (lane == HEAD + 1)).astype(F32)

    @pl.loop(0, frames // TALL, unroll=4)
    def _(block):
        rows = rows_of(block, TALL)
        for part in range(TALL // 32):
            at = pl.ds(pl.multiple_of(block * TALL + part * 32, 32), 32)
            hat = centre_rows(x_ref[at].astype(F32))
            hat_out.buffer[at] = hat.astype(BF16)
            n_attn_out.buffer[at] = (hat * attn_gain + attn_bias).astype(BF16)
            n_mlp_out.buffer[at] = (hat * mlp_gain + mlp_bias).astype(BF16)
        parts = dot_nn(n_attn_out.buffer[rows], qkv_ref[...])
        query = parts[:, :LANES]
        query_out.buffer[rows, :LANES] = ((query + content).astype(BF16).astype(F32) * 0.125).astype(BF16)
        q_position = (query + position).astype(BF16)
        q_position_out.buffer[rows] = q_position
        key_out.buffer[rows, :LANES] = parts[:, LANES : 2 * LANES].astype(BF16)
        value_out.buffer[rows] = (parts[:, 2 * LANES :] + spare).astype(BF16)
        projected = dot_nt(q_position, pos_ref[...])
        for part in range(TALL // 32):
            at = pl.ds(pl.multiple_of(block * TALL + part * 32, 32), 32)
            inner = part * 32 % BLOCK
            sine, cosine = angle_rows(
                coarse_ref, fine_ref, block * (TALL // BLOCK) + part * 32 // BLOCK, slice(inner, inner + 32)
            )
            first = projected[part * 32 : part * 32 + 32, :half]
            second = projected[part * 32 : part * 32 + 32, half:]
            query_out.buffer[at, LANES : LANES + half] = ((first * sine + second * cosine) * 0.125).astype(BF16)
            query_out.buffer[at, LANES + half :] = ((second * sine - first * cosine) * 0.125).astype(BF16)
            key_out.buffer[at, LANES : LANES + half] = cosine.astype(BF16)
            key_out.buffer[at, LANES + half :] = sine.astype(BF16)

    for out in (n_attn_out, n_mlp_out, hat_out, q_position_out, query_out, key_out, value_out):
        out.go()
    up_ref = up_ref()
    up_bias = line_of(up_bias_ref)[:, HALF:]
    @pl.loop(0, frames // TALL, unroll=2)
    def _(block):
        values = dot_nn(n_mlp_out.buffer[rows_of(block, TALL)], up_ref[...])
        for part in range(TALL // 16):
            pre = values[part * 16 : part * 16 + 16] + up_bias
            hidden = pre * (0.5 + 0.5 * lax.erf(pre * math.sqrt(0.5)))
            mean = jnp.mean(hidden, axis=-1, keepdims=True)
            centred = hidden - mean
            rate = lax.rsqrt(jnp.mean(centred * centred, axis=-1, keepdims=True) + EPS)
            at = pl.ds(pl.multiple_of(block * TALL + part * 16, 16), 16)
            mean_out.buffer[at] = jnp.broadcast_to(mean, (16, LANES))
            rate_out.buffer[at] = jnp.broadcast_to(rate, (16, LANES))

    mean_out.go()
    rate_out.go()
    key_code = item_codes(bounds_s, lax.broadcasted_iota(jnp.int32, (1, frames), 1))

    low = low_lanes(32)
    for block in range(frames // TALL):
        rows = pl.ds(block * TALL, TALL)
        raw = dot_nt(query_out.buffer[rows], key_out.buffer[...])
        for part in range(TALL // 32):
            start = block * TALL + part * 32
            index = start + lax.broadcasted_iota(jnp.int32, (32, 1), 0)
            scaled = jnp.where(
                item_codes(bounds_s, index) == key_code, raw[part * 32 : part * 32 + 32], MASKED
            )
            weight = jnp.exp(scaled - jnp.max(scaled, axis=1, keepdims=True))
            prob_out.buffer[pl.ds(start, 32)] = weight.astype(BF16)
        prob_out.go(rows)
        attn = dot_nn(prob_out.buffer[rows], value_out.buffer[...])
        for part in range(TALL // 32):
            own = attn[part * 32 : part * 32 + 32]
            share = 1.0 / own[:, HEAD : HEAD + 1]
            attn_out.buffer[pl.ds(block * TALL + part * 32, 32)] = jnp.where(low, own * share, share)


def fill_margins(wide_s, frames):
    edge = jnp.zeros((MARGIN, LANES), F32)
    wide_s[:MARGIN] = edge
    wide_s[MARGIN + frames : 2 * MARGIN + frames] = edge
    base = frames + 3 * MARGIN
    after = base + frames // 2
    low = low_lanes(MARGIN)
    wide_s[base - MARGIN : base] = jnp.where(low, 0.0, turn(wide_s[after - MARGIN : after]))
    wide_s[after : after + MARGIN] = jnp.where(low, turn(wide_s[base : base + MARGIN]), 0.0)


def item_span(bounds_s, frame):
    begin, end = bounds_s[0], bounds_s[BOUNDS - 1]
    for item in range(1, ITEMS + 1):
        edge = bounds_s[item]
        begin = jnp.where(frame >= edge, edge, begin)
    for item in range(ITEMS, 0, -1):
        edge = bounds_s[item]
        end = jnp.where(frame < edge, edge, end)
    return begin, end


def is_whole(bounds_s, start):
    begin, end = item_span(bounds_s, start)
    reach = KERNEL // 2
    low = (begin == 0) | (begin <= start - reach)
    high = (end == bounds_s[BOUNDS - 1]) | (end >= start + WINDOW + reach)
    return low & high & (end >= start + WINDOW)


def tap_limits(bounds_s, start):
    frame = start + lax.broadcasted_iota(jnp.int32, (WINDOW, LANES), 0)
    begin, end = item_span(bounds_s, frame)
    return begin - frame, end - frame


def grouped(values):
    return values.reshape(WINDOW // 8, 8, LANES)


def triple_places(step, frames):
    half = frames // 2
    return (
        pl.multiple_of(step * WINDOW, 2 * MARGIN),
        pl.multiple_of(step * WINDOW + half, 2 * MARGIN),
        pl.multiple_of(step * WINDOW + frames + 2 * MARGIN, 2 * MARGIN),
    )


def over_windows(bounds_s, frames, body):
    half = frames // 2

    @pl.loop(0, half // WINDOW)
    def _(step):
        start = step * WINDOW
        whole = is_whole(bounds_s, start) & is_whole(bounds_s, start + half)

        @pl.when(whole)
        def _():
            body(step, None)

        @pl.when(jnp.logical_not(whole))
        def _():
            first, second = tap_limits(bounds_s, start), tap_limits(bounds_s, start + half)
            low = low_lanes(WINDOW)
            rest = [jnp.where(low, one, other) for one, other in zip(first, second)]
            body(step, (first, second, rest))


def tap_mask(tap, limits):
    shift = tap - KERNEL // 2
    return None if limits is None else (limits[0] <= shift) & (limits[1] > shift)


def tap_view(window_ref, tap, mask):
    view = window_ref[tap + 1 : tap + 1 + WINDOW]
    return grouped(view if mask is None else jnp.where(mask, view, 0.0))


def mlp_first_kernel(
    lengths_ref,
    n_ref,
    up_ref,
    table_ref,
    mean_ref,
    rate_ref,
    cot_ref,
    merge_ref,
    down_ref,
    attn_ref,
    mixed_out,
    gate_pre_out,
    grad_out,
    rate_out,
    hat_out,
    early_out,
    vectors_out,
    lines_out,
    hat_s,
    slope_s,
    gate_s,
    hidden_s,
    gate_slope_s,
    conv_s,
    grad_s,
    out_s,
    back_s,
    branch_s,
    mix_s,
    taps_s,
    turn_s,
    tap_sum_s,
    columns_s,
    forward_s,
    backward_s,
    bounds_s,
):
    place = lax.axis_index("tm")
    frames = mix_s.shape[0]
    half = frames // 2
    blocks = frames // BLOCK
    quarters, early_rows, _ = early_out.buffer.shape
    share = early_rows // 8
    channels = quarters * share
    fill_bounds(lengths_ref, bounds_s, frames)
    for part in range(2):
        for tap in range(KERNEL):
            line = jnp.broadcast_to(table_ref[part, 8 + tap : 9 + tap], (8, LANES))
            taps_s[part, tap] = line
            turn_s[part, KERNEL - 1 - tap] = line
    tap_sum_s[...] = jnp.zeros(tap_sum_s.shape, F32)
    main, rest = table_ref[0, :8], table_ref[1, :8]
    mixed_bias = jnp.where(low_lanes(1), rest[0:1], rest[1:2])
    low = low_lanes(64)
    gate_pre_ref = gate_pre_out.buffer
    n_ref = n_ref()
    mean_ref, rate_ref = mean_ref(), rate_ref()
    begin(cot_ref, merge_ref, down_ref, attn_ref)

    def stat_rows(rows):
        return mean_ref[rows], rate_ref[rows]

    def chunk(start, base=0):
        return pl.ds(pl.multiple_of(start, 64) + base, 64)

    def conv_part(hidden, mean, rate, lines, rows, to_rows):
        hat = (hidden - mean) * rate
        hat_s[rows] = hat
        hat_out.buffer[rows] = hat.astype(BF16)
        conv_s[to_rows] = (hat * lines[2:3] + lines[3:4]).astype(BF16).astype(F32)

    @pl.loop(0, half // TALL, unroll=2)
    def _(block):
        pre = [dot_nn(n_ref[rows_of(block, TALL, base)], up_ref[...]) for base in (0, half)]
        for part in range(TALL // 64):
            inner = slice(part * 64, part * 64 + 64)
            start = block * TALL + part * 64
            mixed = []
            for values, base in zip(pre, (0, half)):
                rows = chunk(start, base)
                gate, gate_slope = gelu_parts(values[inner, :LANES] + main[0:1])
                hidden_s[rows] = gate
                gate_slope_s[rows] = gate_slope
                hidden, slope = gelu_parts(values[inner, 2 * LANES :] + main[1:2])
                mean, rate = stat_rows(rows)
                slope_s[rows] = slope * rate
                conv_part(hidden, mean, rate, main, rows, chunk(start, base + MARGIN))
                mixed.append((*gelu_parts(values[inner, LANES : 2 * LANES] + mixed_bias), mean, rate))
            (low_hidden, low_slope, low_mean, low_rate), (high_hidden, high_slope, high_mean, high_rate) = mixed
            rows = chunk(start, frames)
            hidden_s[rows] = jnp.where(low, low_hidden, turn(high_hidden))
            gate_slope_s[rows] = jnp.where(low, low_slope, turn(high_slope))
            rate = jnp.where(low, low_rate, high_rate)
            slope_s[rows] = jnp.where(low, turn(low_slope), high_slope) * rate
            conv_part(
                jnp.where(low, turn(low_hidden), high_hidden),
                jnp.where(low, low_mean, high_mean),
                rate,
                rest,
                rows,
                chunk(start, frames + 3 * MARGIN),
            )

    hat_out.go()
    fill_margins(conv_s, frames)
    tall = WINDOW + 2 * MARGIN
    outs = (0, half, frames)

    def convolve(step, limits):
        for index, base in enumerate(triple_places(step, frames)):
            forward_s[index] = conv_s[pl.ds(base, tall)]
        for index in range(3):
            own = None if limits is None else limits[index]
            total = jnp.zeros((WINDOW // 8, 8, LANES), F32)
            for tap in range(KERNEL):
                mask = tap_mask(tap, own)
                total = total + tap_view(forward_s.at[index], tap, mask) * taps_s[index // 2, tap][None]
            lines = rest if index == 2 else main
            out_s[rows_of(step, WINDOW, outs[index])] = total.reshape(WINDOW, LANES) + lines[4:5]

    over_windows(bounds_s, frames, convolve)
    cot_ref = cot_ref()
    merge_ref = merge_ref()
    down_ref = down_ref()
    attn_ref = attn_ref()
    down_ref[channels:] = jnp.zeros((2 * LANES - channels, D), BF16)
    zero = jnp.zeros((8, LANES), F32)

    def branch_part(grad_gated, rows, to_rows, sums):
        up_sum, conv_sum = sums
        gate, conv = hidden_s[rows], out_s[rows]
        gate_pre = (grad_gated * conv * gate_slope_s[rows]).astype(BF16)
        gate_pre_ref[rows] = gate_pre
        grad_conv = (grad_gated * gate).astype(BF16).astype(F32)
        grad_s[to_rows] = grad_conv
        gate_pre = gate_pre.astype(F32)
        return gate * conv, gate_pre, (up_sum + fold_rows(gate_pre), conv_sum + fold_rows(grad_conv))

    def branch_step(block, sums):
        main_sums, rest_sums = sums
        grads = []
        for base in (0, half):
            rows = rows_of(block, TALL, base)
            branch = dot_nt(cot_ref[rows], merge_ref[...]).astype(BF16)
            branch_s[rows] = branch
            grads.append(dot_nt(branch, down_ref[...]))
        for part in range(TALL // 64):
            inner = slice(part * 64, part * 64 + 64)
            start = block * TALL + part * 64
            for values, base in zip(grads, (0, half)):
                rows = chunk(start, base)
                gated, gate_pre, main_sums = branch_part(
                    values[inner, :LANES], rows, chunk(start, base + MARGIN), main_sums
                )
                mix_s[rows, :LANES] = gated.astype(BF16)
                gate_s[rows, :LANES] = gate_pre.astype(BF16)
            grad = jnp.where(low, grads[0][inner, LANES:], turn(grads[1][inner, LANES:]))
            gated, gate_pre, rest_sums = branch_part(
                grad, chunk(start, frames), chunk(start, frames + 3 * MARGIN), rest_sums
            )
            low_rows, high_rows = chunk(start), chunk(start, half)
            gate_s[low_rows, LANES:] = gate_pre.astype(BF16)
            gate_s[high_rows, LANES:] = turn(gate_pre).astype(BF16)
            mix_s[low_rows, LANES:] = jnp.where(low, gated, turn(attn_ref[low_rows])).astype(BF16)
            mix_s[high_rows, LANES:] = jnp.where(low, turn(gated), turn(attn_ref[high_rows])).astype(BF16)
        return main_sums, rest_sums

    (main_up, main_conv), (rest_up, rest_conv) = lax.fori_loop(
        0, half // TALL, branch_step, ((zero, zero), (zero, zero)), unroll=2
    )
    gate_pre_out.go()
    fill_margins(grad_s, frames)
    own = rows_of(place, BLOCK)
    lines_out[0:1] = one_row(fold_rows(branch_s[own].astype(F32)))
    lines_out[1:2] = one_row(fold_rows(cot_ref[own].astype(F32)))
    lines_out[2:8] = jnp.zeros((6, D), F32)
    grad_down = dot_tn(mix_s[...], branch_s[...])
    grad_gate = dot_tn(gate_s[...], n_ref[...])
    for quarter in range(quarters):
        for tile in range(4):
            early_out.buffer[quarter, tile * share : (tile + 1) * share] = grad_down[
                quarter * share : (quarter + 1) * share, tile * LANES : (tile + 1) * LANES
            ].astype(BF16)
        early_out.buffer[quarter, 4 * share :] = grad_gate[
            :channels, quarter * LANES : (quarter + 1) * LANES
        ].astype(BF16)
    early_out.go()
    for block in range(blocks):
        mixed_out.buffer[block, :BLOCK] = mix_s[block * BLOCK : (block + 1) * BLOCK]
    mixed_out.go(slice(None), pl.ds(0, BLOCK))

    def differentiate(step, limits):
        for index, base in enumerate(triple_places(step, frames)):
            forward_s[index] = conv_s[pl.ds(base, tall)]
            backward_s[index] = grad_s[pl.ds(base, tall)]
        for index in range(3):
            own = None if limits is None else limits[index]
            total = jnp.zeros((WINDOW // 8, 8, LANES), F32)
            centre = grouped(backward_s[index, MARGIN : MARGIN + WINDOW])
            for tap in range(KERNEL):
                mask = tap_mask(tap, own)
                total = total + tap_view(backward_s.at[index], tap, mask) * turn_s[index // 2, tap][None]
                tap_sum_s[index // 2, tap] += jnp.sum(tap_view(forward_s.at[index], tap, mask) * centre, axis=0)
            back_s[rows_of(step, WINDOW, outs[index])] = total.reshape(WINDOW, LANES)

    over_windows(bounds_s, frames, differentiate)
    lane = lax.broadcasted_iota(jnp.int32, (64, LANES), 1)

    def norm_part(rows, lines, sums):
        gain_sum, bias_sum = sums
        back, hat, slope = back_s[rows], hat_s[rows], slope_s[rows]
        grad = back * lines[2:3]
        grad_out.buffer[rows] = (grad * slope).astype(BF16)
        rate_out.buffer[rows] = slope.astype(BF16)
        along = back * hat
        return grad, along * lines[2:3], (gain_sum + fold_rows(along), bias_sum + fold_rows(back))

    def norm_step(block, sums):
        main_sums, rest_sums = sums
        for part in range(TALL // 64):
            start = block * TALL + part * 64
            pairs = []
            for base in (0, half):
                plain, along, main_sums = norm_part(chunk(start, base), main, main_sums)
                pairs.append([plain, along])
            plain, along, rest_sums = norm_part(chunk(start, frames), rest, rest_sums)
            for item, values in enumerate((plain, along)):
                pairs[0][item] = pairs[0][item] + jnp.where(low, values, 0.0)
                pairs[1][item] = pairs[1][item] + jnp.where(low, 0.0, values)
            for (plain, along), base in zip(pairs, (0, half)):
                columns_s[chunk(start, base)] = jnp.where(
                    lane == 0,
                    jnp.sum(plain, axis=-1, keepdims=True),
                    jnp.where(lane == 1, jnp.sum(along, axis=-1, keepdims=True), 0.0),
                )
        return main_sums, rest_sums

    (main_gain, main_bias), (rest_gain, rest_bias) = lax.fori_loop(
        0, half // TALL, norm_step, ((zero, zero), (zero, zero)), unroll=2
    )
    grad_out.go()
    rate_out.go()
    totals = jnp.concatenate(
        [jnp.transpose(columns_s[block * BLOCK : (block + 1) * BLOCK])[:2] for block in range(blocks)], axis=0
    )
    high = totals.astype(BF16)
    low_part = (totals - high.astype(F32)).astype(BF16)
    for block in range(blocks):
        mixed_out.buffer[block, BLOCK:, :LANES] = high
        mixed_out.buffer[block, BLOCK:, LANES:] = low_part
    mixed_out.go(slice(None), pl.ds(BLOCK, 2 * blocks))

    def vectors(part, lines):
        taps = jnp.sum(tap_sum_s[part], axis=1)[:KERNEL]
        stacked = jnp.concatenate([taps] + [one_row(line) for line in lines], axis=0)
        if part:
            stacked = stacked + turn(stacked)
        return jnp.transpose(
            jnp.concatenate([stacked, jnp.zeros((LANES - stacked.shape[0], LANES), F32)], axis=0)
        )

    vectors_out[:LANES] = vectors(0, (main_conv, main_gain, main_bias, main_up))
    vectors_out[LANES:] = vectors(1, (rest_conv, rest_gain, rest_bias, rest_up))[: channels - LANES]


def attend_back_kernel(
    cot_ref,
    merge_ref,
    head_ref,
    attn_ref,
    value_ref,
    prob_ref,
    key_ref,
    coarse_ref,
    fine_ref,
    pos_ref,
    query_ref,
    n_ref,
    q_position_ref,
    qkv_ref,
    hat_ref,
    gain_ref,
    early_ref,
    branch_out,
    total_out,
    pack_0,
    pack_1,
    pack_2,
    pack_3,
    lines_out,
    grad_s,
    raw_s,
    projected_s,
    parts_s,
    grads_s,
):
    place = lax.axis_index("tm")
    frames = raw_s.shape[0]
    blocks = frames // BLOCK
    half = D // 2
    zero = jnp.zeros((8, LANES), F32)
    cot_ref, merge_ref, head_ref, attn_ref = cot_ref(), merge_ref(), head_ref(), attn_ref()
    head_ref[HEAD:] = jnp.zeros((LANES - HEAD, D), BF16)
    begin(value_ref, prob_ref, key_ref, pos_ref)

    @pl.loop(0, frames // TALL, unroll=4)
    def _(block):
        rows = rows_of(block, TALL)
        branch = dot_nt(cot_ref[rows], merge_ref[...]).astype(BF16)
        branch_out.buffer[rows] = branch
        grad = (dot_nt(branch, head_ref[...]) * attn_ref[rows, HEAD : HEAD + 1]).astype(BF16).astype(F32)
        delta = jnp.sum(grad * attn_ref[rows], axis=1, keepdims=True)
        high = delta.astype(BF16).astype(F32)
        lane = lax.broadcasted_iota(jnp.int32, (TALL, LANES), 1)
        grad = jnp.where(lane == HEAD, -high, jnp.where(lane == HEAD + 1, high - delta, grad))
        grad_s[rows] = grad.astype(BF16)

    branch_out.go()
    value_ref, prob_ref = value_ref(), prob_ref()
    key_ref, pos_ref = key_ref(), pos_ref()
    begin(query_ref, n_ref, q_position_ref, qkv_ref, hat_ref, early_ref)

    def score_step(block, sums):
        content_sum, position_sum = sums
        rows = rows_of(block, TALL)
        grad = grad_s[rows]
        score = dot_nt(grad, value_ref[...])
        for part in range(TALL // 32):
            at = pl.ds(pl.multiple_of(block * TALL + part * 32, 32), 32)
            inner = slice(part * 32, part * 32 + 32)
            raw_s[at] = (prob_ref[at].astype(F32) * score[inner]).astype(BF16)
        query = dot_nn(raw_s[rows], key_ref[...]) * 0.125
        for part in range(TALL // 32):
            at = pl.ds(pl.multiple_of(block * TALL + part * 32, 32), 32)
            inner = part * 32 % BLOCK
            sine, cosine = angle_rows(
                coarse_ref, fine_ref, block * (TALL // BLOCK) + part * 32 // BLOCK, slice(inner, inner + 32)
            )
            inner = slice(part * 32, part * 32 + 32)
            first, second = query[inner, LANES : LANES + half], query[inner, LANES + half :]
            projected_s[at, :half] = (first * sine - second * cosine).astype(BF16)
            projected_s[at, half:] = (first * cosine + second * sine).astype(BF16)
        position = dot_nn(projected_s[rows], pos_ref[...])
        content = query[:, :LANES]
        parts_s[rows, :LANES] = (content + position).astype(BF16)
        return content_sum + fold_rows(content), position_sum + fold_rows(position)

    content_sum, position_sum = lax.fori_loop(0, frames // TALL, score_step, (zero, zero), unroll=4)
    query_ref, n_ref, q_position_ref = query_ref(), n_ref(), q_position_ref()
    qkv_ref, hat_ref = qkv_ref(), hat_ref()
    grad_key = dot_tn(query_ref[...], raw_s[...])
    grad_value = dot_tn(grad_s[...], prob_ref[...])
    for block in range(blocks):
        at = slice(block * BLOCK, (block + 1) * BLOCK)
        parts_s[at, LANES : 2 * LANES] = jnp.transpose(grad_key[:, at]).astype(BF16)
        parts_s[at, 2 * LANES :] = jnp.transpose(grad_value[:, at]).astype(BF16)
    grads_s[:HEAD] = dot_tn(parts_s[:, :LANES], n_ref[...])[:HEAD]
    grads_s[HEAD : 2 * HEAD] = dot_nn(grad_key.astype(BF16), n_ref[...])[:HEAD]
    grads_s[2 * HEAD : 3 * HEAD] = dot_nn(grad_value.astype(BF16), n_ref[...])[:HEAD]
    grads_s[3 * HEAD :] = dot_tn(q_position_ref[...], projected_s[...])[:HEAD]
    stream = lax.axis_index("stream")
    early_ref = early_ref()
    for apart, pack_out in enumerate((pack_0, pack_1, pack_2, pack_3)):
        quarter = lax.bitwise_xor(stream, jnp.int32(apart))
        lanes = pl.ds(pl.multiple_of(quarter * LANES, LANES), LANES)
        pack_out.buffer[: 4 * HEAD] = grads_s[:, lanes].astype(BF16)
        pack_out.buffer[4 * HEAD :] = early_ref[quarter]
        pack_out.go()
    gain = line_of(gain_ref)
    wide_zero = jnp.zeros((8, D), F32)

    def norm_step(block, sums):
        gain_sum, bias_sum = sums
        grad = dot_nt(parts_s[rows_of(block, TALL)], qkv_ref[...])
        for part in range(TALL // 32):
            at = pl.ds(pl.multiple_of(block * TALL + part * 32, 32), 32)
            own = grad[part * 32 : part * 32 + 32]
            total_out.buffer[at] = (own * gain).astype(BF16)
            gain_sum = gain_sum + fold_rows(own * hat_ref[at].astype(F32))
            bias_sum = bias_sum + fold_rows(own)
        return gain_sum, bias_sum

    gain_sum, bias_sum = lax.fori_loop(0, frames // TALL, norm_step, (wide_zero, wide_zero), unroll=4)
    lane = lax.broadcasted_iota(jnp.int32, (1, LANES), 1)

    def own_lanes(sums):
        line = one_row(sums)
        line = line + turn(line)
        tiles = [
            jnp.where(lax.div(tile * LANES + lane, HEAD) == place, line, 0.0) for tile in range(D // LANES)
        ]
        return jnp.concatenate(tiles, axis=1)

    lines_out[...] = jnp.concatenate(
        [
            one_row(gain_sum),
            one_row(bias_sum),
            own_lanes(content_sum),
            own_lanes(position_sum),
            jnp.zeros((4, D), F32),
        ],
        axis=0,
    )


def mlp_second_kernel(
    mixed_ref,
    gate_pre_ref,
    grad_ref,
    rate_ref,
    hat_ref,
    up_ref,
    norm_hat_ref,
    gain_ref,
    other_ref,
    pre_out,
    same_out,
    apart_out,
    lines_out,
    up_out,
    columns_s,
):
    place = lax.axis_index("tm")
    pre_s = pre_out.buffer
    frames = pre_s.shape[0]
    half = frames // 2
    blocks = frames // BLOCK
    totals = jnp.zeros((2 * blocks, LANES), F32)
    mixed_ref = mixed_ref()
    for source in range(mixed_ref.shape[0]):
        both = mixed_ref[source].astype(F32)
        totals = totals + (both[:, :LANES] + both[:, LANES:])
    totals = totals * (1.0 / HALF)
    high = totals.astype(BF16)
    low_part = (totals - high.astype(F32)).astype(BF16)
    both = jnp.concatenate([high, low_part], axis=0)
    lane = lax.broadcasted_iota(jnp.int32, (4 * blocks, 2 * LANES), 1) // LANES
    line = lax.broadcasted_iota(jnp.int32, (4 * blocks, 2 * LANES), 0)
    for block in range(blocks):
        chosen = (lax.rem(line, 2 * blocks) == 2 * block + lane).astype(F32).astype(BF16)
        columns_s[block * BLOCK : (block + 1) * BLOCK] = dot_tn(both, chosen)
    gate_pre_ref, grad_ref, rate_ref, hat_ref = gate_pre_ref(), grad_ref(), rate_ref(), hat_ref()
    begin(up_ref, norm_hat_ref, other_ref)
    low = low_lanes(64)
    gain = line_of(gain_ref)

    def chunk(start, base=0):
        return pl.ds(pl.multiple_of(start, 64) + base, 64)

    def pre_part(rows, table, up_sum):
        plain, along = table
        hat, rate = hat_ref[rows].astype(F32), rate_ref[rows].astype(F32)
        pre = (grad_ref[rows].astype(F32) - rate * (plain + hat * along)).astype(BF16).astype(F32)
        return pre, up_sum + fold_rows(pre)

    def pre_step(block, sums):
        main_up, rest_up = sums
        for part in range(TALL // 64):
            start = block * TALL + part * 64
            tables = []
            for base in (0, half):
                rows = chunk(start, base)
                table = [columns_s[rows, item * LANES : (item + 1) * LANES] for item in range(2)]
                tables.append(table)
                pre, main_up = pre_part(rows, table, main_up)
                pre_s[rows, :LANES] = gate_pre_ref[rows]
                pre_s[rows, 2 * LANES :] = pre.astype(BF16)
            rows = chunk(start, frames)
            table = [jnp.where(low, one, other) for one, other in zip(*tables)]
            pre, rest_up = pre_part(rows, table, rest_up)
            gate_pre = gate_pre_ref[rows].astype(F32)
            pre_s[chunk(start), LANES : 2 * LANES] = jnp.where(low, gate_pre, turn(pre)).astype(BF16)
            pre_s[chunk(start, half), LANES : 2 * LANES] = jnp.where(low, turn(gate_pre), pre).astype(BF16)
        return main_up, rest_up

    zero = jnp.zeros((8, LANES), F32)
    main_up, rest_up = lax.fori_loop(0, half // TALL, pre_step, (zero, zero), unroll=2)
    pre_out.go()
    up_ref, norm_hat_ref, other_ref = up_ref(), norm_hat_ref(), other_ref()
    wide_zero = jnp.zeros((8, D), F32)

    def norm_step(step, sums):
        gain_sum, bias_sum = sums
        grads = dot_nt(pre_s[rows_of(step, TALL)], up_ref[...])
        for part in range(TALL // BLOCK):
            block = step * (TALL // BLOCK) + part
            rows = rows_of(block, BLOCK)
            grad = grads[part * BLOCK : (part + 1) * BLOCK]
            total = (grad * gain + other_ref[rows].astype(F32)).astype(BF16)
            apart = lax.bitwise_xor(block, place)

            @pl.when(lax.rem(apart, 2) == 0)
            def _(apart=apart, total=total):
                same_out.buffer[lax.div(apart, 2)] = total

            @pl.when(lax.rem(apart, 2) == 1)
            def _(apart=apart, total=total):
                apart_out.buffer[lax.div(apart, 2)] = total

            gain_sum = gain_sum + fold_rows(grad * norm_hat_ref[rows].astype(F32))
            bias_sum = bias_sum + fold_rows(grad)
        return gain_sum, bias_sum

    gain_sum, bias_sum = lax.fori_loop(0, frames // TALL, norm_step, (wide_zero, wide_zero), unroll=2)
    apart_out.go()
    same_out.go()
    lines_out[...] = jnp.concatenate([one_row(gain_sum), one_row(bias_sum), jnp.zeros((6, D), F32)], axis=0)
    rest_line = one_row(rest_up)
    up_out[:LANES] = jnp.transpose(jnp.broadcast_to(one_row(main_up), (LANES, LANES)))
    up_out[LANES:] = jnp.transpose(jnp.broadcast_to(rest_line + turn(rest_line), (LANES, LANES)))[:LOW]


def late_pack_kernel(
    pre_ref,
    n_ref,
    joined_ref,
    branch_ref,
    cot_ref,
    vectors_ref,
    up_columns_ref,
    first_lines_ref,
    head_lines_ref,
    own_lines_ref,
    pack_out,
):
    pack_ref = pack_out.buffer
    quarters = pack_ref.shape[0]
    channels = vectors_ref.shape[0]
    share = channels // quarters
    gate_at = KERNEL + 3
    lane = lax.broadcasted_iota(jnp.int32, (share, LANES), 1)
    lines = jnp.concatenate(
        [
            head_lines_ref[0:2],
            own_lines_ref[0:2],
            head_lines_ref[2:4],
            first_lines_ref[0:2],
            jnp.zeros((8, D), F32),
        ],
        axis=0,
    )
    for quarter in range(quarters):
        table = vectors_ref[quarter * share : (quarter + 1) * share]
        for other in range(2):
            at = slice((2 * (quarter % 2) + other) * share, (2 * (quarter % 2) + other + 1) * share)
            column = vectors_ref[at, gate_at : gate_at + 1] if quarter < quarters // 2 else up_columns_ref[at, 0:1]
            table = jnp.where(lane == gate_at + other, column, table)
        pack_ref[quarter, channels : channels + share] = table.astype(BF16)
        pack_ref[quarter, channels + share : channels + share + 16] = lines[
            :, quarter * LANES : (quarter + 1) * LANES
        ].astype(BF16)
    grad_up = dot_tn(pre_ref()[...], n_ref()[...])
    for quarter in range(quarters):
        lanes = slice(quarter * LANES, (quarter + 1) * LANES)
        pack_ref[quarter, :LANES] = grad_up[LANES:, lanes].astype(BF16)
        pack_ref[quarter, LANES:channels] = grad_up[LOW:LANES, lanes].astype(BF16)
    joined_ref, cot_ref, branch_ref = joined_ref(), cot_ref(), branch_ref()
    sources, _, rows = joined_ref.shape
    merge_rows = 2 * D // sources
    head_rows = D // sources
    grad_merge = jnp.zeros((merge_rows, D), F32)
    grad_head = jnp.zeros((head_rows, D), F32)
    for source in range(sources):
        at = slice(source * rows, (source + 1) * rows)
        joined = joined_ref[source]
        grad_merge = grad_merge + dot_nn(joined[:merge_rows], cot_ref[at])
        grad_head = grad_head + dot_nn(joined[merge_rows : merge_rows + head_rows], branch_ref[at])
    for quarter in range(quarters):
        base = channels + share + 16
        for grad in (grad_merge, grad_head):
            part = grad.shape[0] // quarters
            for tile in range(4):
                pack_ref[quarter, base : base + part] = grad[
                    quarter * part : (quarter + 1) * part, tile * LANES : (tile + 1) * LANES
                ].astype(BF16)
                base += part


def output_kernel(
    x_ref, mixed_ref, head_ref, down_ref, down_bias_ref, merge_ref, merge_bias_ref, out_ref, joined_out
):
    sources = mixed_ref.shape[0]
    rows = x_ref.shape[0]
    channels = HALF // sources
    share = channels // 4
    attn_parts = []
    branch_attn = jnp.zeros((rows, D), F32)
    branch_mlp = jnp.zeros((rows, D), F32)
    for source in range(sources):
        attn = turn(mixed_ref[source, :rows, LANES:].astype(F32))[:, :HEAD].astype(BF16)
        attn_parts.append(attn)
        branch_attn = branch_attn + dot_nn(attn, head_ref[source * HEAD : (source + 1) * HEAD])
        down = jnp.concatenate(
            [down_ref[(part * sources + source) * share : (part * sources + source + 1) * share] for part in range(4)],
            axis=0,
        )
        branch_mlp = branch_mlp + dot_nn(mixed_ref[source, :rows, :channels], down)
    joined = jnp.concatenate(
        [branch_attn.astype(BF16), (branch_mlp + line_of(down_bias_ref)).astype(BF16)], axis=1
    )
    result = x_ref[...].astype(F32) + dot_nn(joined, merge_ref[...]) + line_of(merge_bias_ref)
    out_ref[...] = result.astype(BF16)
    turned = jnp.transpose(joined.astype(F32))
    heads = jnp.transpose(jnp.concatenate(attn_parts, axis=1).astype(F32))
    merge_share = turned.shape[0] // (4 * sources)
    head_share = heads.shape[0] // (4 * sources)
    used = 4 * (merge_share + head_share)
    for target in range(sources):
        for part in range(4):
            at = (part * sources + target) * merge_share
            joined_out[target, part * merge_share : (part + 1) * merge_share] = turned[
                at : at + merge_share
            ].astype(BF16)
            at = (part * sources + target) * head_share
            to = 4 * merge_share + part * head_share
            joined_out[target, to : to + head_share] = heads[at : at + head_share].astype(BF16)
        joined_out[target, used:] = jnp.zeros((joined_out.shape[1] - used, rows), BF16)


def pair_kernel(same_ref, other_ref, *out_refs):
    for slot, out_ref in enumerate(out_refs):
        out_ref[...] = (same_ref[slot].astype(F32) + other_ref[slot].astype(F32)).astype(BF16)


def frames_kernel(x_ref, cot_ref, *refs):
    total_refs, out_ref = refs[:-1], refs[-1]
    for part in range(x_ref.shape[0] // 32):
        rows = slice(part * 32, part * 32 + 32)
        inputs = x_ref[rows].astype(F32)
        mean = jnp.mean(inputs, axis=-1, keepdims=True)
        centred = inputs - mean
        rate = lax.rsqrt(jnp.mean(centred * centred, axis=-1, keepdims=True) + EPS)
        hat = centred * rate
        grad = total_refs[0][rows].astype(F32)
        for total_ref in total_refs[1:]:
            grad = grad + total_ref[rows].astype(F32)
        plain = jnp.mean(grad, axis=-1, keepdims=True)
        along = jnp.mean(grad * hat, axis=-1, keepdims=True)
        out_ref[rows] = cot_ref[rows].astype(F32) + rate * (grad - plain - hat * along)


def add_kernel(*refs):
    out_ref = refs[-1]
    first = 0
    for at in range(0, len(refs) - 1, 4):
        total = refs[at][...].astype(F32)
        for ref in refs[at + 1 : at + 4]:
            total = total + ref[...].astype(F32)
        out_ref[first : first + total.shape[0]] = total.astype(BF16)
        first += total.shape[0]


def gather_parts(near_ref, far_ref, all_s):
    place = lax.axis_index("tm")
    for apart in range(all_s.shape[0]):
        part_ref = far_ref if apart % 2 else near_ref
        all_s[lax.bitwise_xor(jnp.int32(apart), place)] = part_ref[apart // 2]


def lines_from(all_s, base, size):
    return jnp.concatenate([all_s[source, base : base + size] for source in range(all_s.shape[0])], axis=0).astype(F32)


def add_streams_kernel(parts_ref, out_ref):
    total = parts_ref[0].astype(F32)
    for source in range(1, parts_ref.shape[0]):
        total = total + parts_ref[source].astype(F32)
    out_ref[...] = total.astype(BF16)


def early_kernel(near_ref, far_ref, qkv_out, pos_out, down_out, up_out, all_s):
    gather_parts(near_ref, far_ref, all_s)
    sources = all_s.shape[0]
    share = HALF // (4 * sources)
    for kind in range(4):
        lines = jnp.transpose(lines_from(all_s, kind * HEAD, HEAD))
        if kind < 3:
            qkv_out[:, kind * D : (kind + 1) * D] = lines
        else:
            pos_out[...] = lines
    base = 4 * HEAD
    for source in range(sources):
        for tile in range(4):
            down_out[source * share : (source + 1) * share, tile * LANES : (tile + 1) * LANES] = all_s[
                source, base + tile * share : base + (tile + 1) * share
            ].astype(F32)
    wide = sources * share
    for group in range(4):
        up_out.buffer[:, group * wide : (group + 1) * wide] = jnp.transpose(
            lines_from(all_s, base + 4 * share + group * share, share)
        )


def late_kernel(*refs):
    _, near_ref, far_ref = refs[:3]
    (
        attn_gain_out,
        attn_bias_out,
        mlp_gain_out,
        mlp_bias_out,
        content_out,
        position_out,
        outw_out,
        up_out,
        up_bias_out,
        gain_out,
        bias_out,
        taps_out,
        conv_bias_out,
        down_bias_out,
        merge_out,
        merge_bias_out,
        all_s,
    ) = refs[3:]
    gather_parts(near_ref, far_ref, all_s)
    sources = all_s.shape[0]
    channels = HALF // sources
    share = channels // 4
    base = 0
    for group in range(4):
        at = group * sources * share
        up_out.buffer[:, at : at + sources * share] = jnp.transpose(lines_from(all_s, base + group * share, share))
    up_out.go()
    table = jnp.transpose(lines_from(all_s, base + channels, share))
    taps_out[...] = table[:KERNEL]
    conv_bias_out[...] = table[KERNEL]
    gain_out[...] = table[KERNEL + 1]
    bias_out[...] = table[KERNEL + 2]
    wide = sources * share
    up_bias_out[:wide] = table[KERNEL + 3]
    up_bias_out[wide:] = table[KERNEL + 4]
    base = base + channels + share
    lines = all_s[0, base : base + 16].astype(F32)
    for source in range(1, sources):
        lines = lines + all_s[source, base : base + 16].astype(F32)
    outs = (attn_gain_out, attn_bias_out, mlp_gain_out, mlp_bias_out, content_out, position_out, down_bias_out, merge_bias_out)
    for line, out in enumerate(outs):
        out[...] = lines[line]
    base = base + 16
    merge_share = 2 * D // (4 * sources)
    head_share = D // (4 * sources)
    for source in range(sources):
        for tile in range(4):
            lanes = slice(tile * LANES, (tile + 1) * LANES)
            at = base + tile * merge_share
            merge_out[source * merge_share : (source + 1) * merge_share, lanes] = all_s[
                source, at : at + merge_share
            ].astype(F32)
            at = base + 4 * merge_share + tile * head_share
            outw_out[source * head_share : (source + 1) * head_share, lanes] = all_s[
                source, at : at + head_share
            ].astype(F32)


def moved(block, axis, bits):
    count = lax.axis_size(axis)
    return lax.ppermute(block, axis, [(index, index ^ bits) for index in range(count)])


def over_streams(packs):
    return [packs[0]] + [moved(packs[bits], "stream", bits) for bits in range(1, lax.axis_size("stream"))]


def near_blocks(block):
    return [block] + [moved(block, "tm", bits) for bits in range(2, lax.axis_size("tm"), 2)]


def far_blocks(near):
    far = [moved(part, "tm", 1) for part in near]
    return [part for pair in zip(near, far) for part in pair]


def far_stack(near):
    stack = jnp.stack(near)
    return stack, moved(stack, "tm", 1)


def head_device(
    frames,
    lengths,
    cotangent,
    ln_attn_gain,
    ln_attn_bias,
    ln_mlp_gain,
    ln_mlp_bias,
    qkv_weight,
    content_bias,
    position_bias,
    pos_weight,
    out_weight,
    up_weight,
    up_bias,
    gate_norm_gain,
    gate_norm_bias,
    conv_kernel,
    conv_bias,
    down_weight,
    down_bias,
    merge_weight,
    merge_bias,
):
    count = lax.axis_size("tm")
    quarters = lax.axis_size("stream")
    own = frames.shape[1]
    total = own * count
    folded = total + total // 2
    padded = folded + 4 * MARGIN
    share = HALF // (quarters * count)
    channels = HALF // count
    quarter = D // quarters
    own_frames = frames[0]
    own_cotangent = cotangent[0]

    whole, late = Part(), Part(late=True)
    near = near_blocks(jnp.concatenate([own_frames, own_cotangent], axis=1))
    up_own, table, qkv_own, pos_own, bias_own = kernel_call(
        select_kernel,
        [
            ((D, 3 * LANES), BF16),
            ((2, 8 + KERNEL + 1, LANES), F32),
            ((D, 3 * LANES), BF16),
            ((D, LANES), BF16),
            ((8, LANES), F32),
        ],
        10 * "v",
    )(
        up_weight,
        up_bias,
        gate_norm_gain,
        gate_norm_bias,
        conv_bias,
        conv_kernel,
        qkv_weight,
        pos_weight,
        content_bias,
        position_bias,
    )
    frequency = jnp.exp(jnp.arange(D // 2, dtype=F32) * (-2.0 * math.log(10000.0) / D))
    coarse = jnp.arange(0, total, BLOCK, dtype=F32)[:, None] * frequency[None]
    fine = jnp.arange(BLOCK, dtype=F32)[:, None] * frequency[None]
    coarse_table = jnp.concatenate([jnp.sin(coarse), jnp.cos(coarse)], axis=1)
    fine_table = jnp.concatenate([jnp.sin(fine), jnp.cos(fine)], axis=1)
    near, up_own, coarse_table, fine_table = lax.optimization_barrier((near, up_own, coarse_table, fine_table))
    blocks = far_blocks(near)

    n_attn, n_mlp, hat, q_position, query, key, value, prob, attn, mean, rate = kernel_call(
        attend_kernel,
        [
            ((total, D), BF16, 1),
            ((total, D), BF16, 1),
            ((total, D), BF16, 1),
            ((total, LANES), BF16, 1),
            ((total, LANES + D), BF16, 1),
            ((total, LANES + D), BF16, 1),
            ((total, LANES), BF16, 1),
            ((total, total), BF16, 1),
            ((total, LANES), F32, 1),
            ((total, LANES), F32, 1),
            ((total, LANES), F32, 1),
        ],
        [
            "s",
            blocks_part(0),
            *"vvvvvvvvv",
            Part((D, HALF), lambda refs, buffer: [(refs[0].at[:, pl.ds(HALF, HALF)], buffer)], late=True),
            "v",
        ],
        bounds=True,
    )(
        lengths,
        *blocks,
        ln_attn_gain,
        ln_attn_bias,
        ln_mlp_gain,
        ln_mlp_bias,
        qkv_own,
        pos_own,
        bias_own,
        coarse_table,
        fine_table,
        up_weight,
        up_bias,
    )

    def own_down(refs, buffer):
        place = lax.axis_index("tm")
        stride = HALF // quarters
        return [
            (
                refs[0].at[pl.ds(pl.multiple_of(part * stride + share * place, 16), share)],
                buffer.at[pl.ds(part * share, share)],
            )
            for part in range(quarters)
        ]

    mixed, gate_pre, grad_y, slope, gate_hat, early_pack, vectors, first_lines = kernel_call(
        mlp_first_kernel,
        [
            ((count, own + 16, 2 * LANES), BF16, 1),
            ((folded, LANES), BF16, 1),
            ((folded, LANES), BF16, 1),
            ((folded, LANES), BF16, 1),
            ((folded, LANES), BF16, 1),
            ((quarters, 8 * share, LANES), BF16, 1),
            ((channels, LANES), F32),
            ((8, D), F32),
        ],
        [
            "s",
            whole,
            "v",
            "v",
            whole,
            whole,
            blocks_part(1, late=True),
            rows_part(D, D, late=True),
            Part((2 * LANES, D), own_down, late=True),
            Part(late=True),
        ],
        [
            ((folded, LANES), F32),
            ((folded, LANES), F32),
            ((total, 2 * LANES), BF16),
            ((folded, LANES), F32),
            ((folded, LANES), F32),
            ((padded, LANES), F32),
            ((padded, LANES), F32),
            ((folded, LANES), F32),
            ((folded, LANES), F32),
            ((total, D), BF16),
            ((total, 2 * LANES), BF16),
            ((2, 32, 8, LANES), F32),
            ((2, 32, 8, LANES), F32),
            ((2, 32, 8, LANES), F32),
            ((total, LANES), F32),
            ((3, WINDOW + 2 * MARGIN, LANES), F32),
            ((3, WINDOW + 2 * MARGIN, LANES), F32),
        ],
        bounds=True,
    )(lengths, n_mlp, up_own, table, mean, rate, *blocks, merge_weight, down_weight, attn)
    mixed_own = lax.all_to_all(mixed, "tm", 0, 0, tiled=True)

    def own_head(refs, buffer):
        at = pl.ds(pl.multiple_of(lax.axis_index("tm") * HEAD, HEAD), HEAD)
        return [(refs[0].at[at], buffer.at[pl.ds(0, HEAD)])]

    branch, from_attn, *head_packs, head_lines = kernel_call(
        attend_back_kernel,
        [
            ((total, D), BF16, 1),
            ((total, D), BF16, 1),
            *([((4 * HEAD + 8 * share, LANES), BF16, 1)] * quarters),
            ((8, D), F32),
        ],
        [
            blocks_part(1),
            rows_part(0, D),
            Part((LANES, D), own_head),
            whole,
            late,
            late,
            late,
            "v",
            "v",
            late,
            Part((total, LANES), lambda refs, buffer: [(refs[0].at[:, pl.ds(0, LANES)], buffer)], late=True),
            late,
            late,
            late,
            late,
            "v",
            late,
        ],
        [
            ((total, LANES), BF16),
            ((total, total), BF16),
            ((total, D), BF16),
            ((total, 3 * LANES), BF16),
            ((4 * HEAD, D), F32),
        ],
    )(
        *blocks,
        merge_weight,
        out_weight,
        attn,
        value,
        prob,
        key,
        coarse_table,
        fine_table,
        pos_own,
        query,
        n_attn,
        q_position,
        qkv_own,
        hat,
        ln_attn_gain,
        early_pack,
    )
    head_parts = over_streams(head_packs)
    mixed_own, _ = lax.optimization_barrier((mixed_own, head_lines))
    out_rows, joined = kernel_call(
        output_kernel,
        [((own, D), BF16), ((count, 256, own), BF16)],
        "vvvvvvv",
        megas=24,
    )(own_frames, mixed_own, out_weight, down_weight, down_bias, merge_weight, merge_bias)
    joined_all = lax.all_to_all(joined, "tm", 0, 0, tiled=True)
    gate_pre, _ = lax.optimization_barrier((gate_pre, joined))
    late_rows = 5 * share + 16 + 3 * D // count
    pre, same, apart, own_lines, up_columns = kernel_call(
        mlp_second_kernel,
        [
            ((total, 3 * LANES), BF16, 1),
            ((count // 2, own, D), BF16, 1),
            ((count // 2, own, D), BF16, 1),
            ((8, D), F32),
            ((channels, LANES), F32),
        ],
        [
            Part(
                (count, 2 * total // BLOCK, 2 * LANES),
                lambda refs, buffer: [(refs[0].at[:, pl.ds(own, 2 * total // BLOCK)], buffer)],
            ),
            *([whole] * 4),
            late,
            late,
            "v",
            late,
        ],
        [((total, 2 * LANES), F32)],
    )(mixed_own, gate_pre, grad_y, slope, gate_hat, up_own, hat, ln_mlp_gain, from_attn)
    sibling = moved(apart, "tm", 1)
    pre, joined_all = lax.optimization_barrier((pre, joined_all))
    (late_pack,) = kernel_call(
        late_pack_kernel,
        [((quarters, late_rows, LANES), BF16, 1)],
        [
            Part(
                (total, 2 * LANES),
                lambda refs, buffer: [(refs[0].at[:, pl.ds(LANES, 2 * LANES)], buffer)],
            ),
            whole,
            whole,
            whole,
            blocks_part(1),
            *"vvvvv",
        ],
    )(pre, n_mlp, joined_all, branch, *blocks, vectors, up_columns, first_lines, head_lines, own_lines)
    late_pack, head_parts = lax.optimization_barrier((late_pack, head_parts))
    late_moved = lax.all_to_all(late_pack, "stream", 0, 0, tiled=True)
    (early_part,) = kernel_call(add_kernel, [((4 * HEAD + 8 * share, LANES), BF16)], quarters * "v", megas=24)(
        *head_parts
    )
    early_near = near_blocks(early_part)
    pairs = kernel_call(pair_kernel, [((own, D), BF16)] * (count // 2), "vv", megas=24)(same, sibling)
    sums = [pairs[0]] + [moved(pairs[slot], "tm", 2 * slot) for slot in range(1, count // 2)]
    late_moved, early_near, sums[1], sums[2] = lax.optimization_barrier((late_moved, early_near, sums[1], sums[2]))
    (late_part,) = kernel_call(add_streams_kernel, [((late_rows, LANES), BF16)], "v", megas=24)(late_moved)
    late_near = near_blocks(late_part)
    early_all = far_stack(early_near)
    grad_qkv, grad_pos, grad_down, half_up = kernel_call(
        early_kernel,
        [
            ((quarter, 3 * D), F32),
            ((quarter, D), F32),
            ((HALF // quarters, D), F32),
            ((quarter, 2 * HALF), F32, 1, (quarter, HALF), lambda ref: ref.at[:, pl.ds(0, HALF)]),
        ],
        "vv",
        [((count, 4 * HEAD + 8 * share, LANES), BF16)],
        megas=24,
    )(*early_all)
    late_near, grad_pos, sums = lax.optimization_barrier((late_near, grad_pos, sums))
    late_parts = far_stack(late_near)
    (grad_frames,) = kernel_call(frames_kernel, [((own, D), F32)], (2 + count // 2) * "v", megas=24)(
        own_frames, own_cotangent, *sums
    )
    late_parts, grad_frames = lax.optimization_barrier((late_parts, grad_frames))
    late = kernel_call(
        late_kernel,
        [((quarter,), F32)] * 6
        + [
            ((quarter, D), F32),
            ((quarter, 2 * HALF), F32, 1, (quarter, HALF), lambda ref: ref.at[:, pl.ds(HALF, HALF)]),
            ((2 * HALF // quarters,), F32),
            ((HALF // quarters,), F32),
            ((HALF // quarters,), F32),
            ((KERNEL, HALF // quarters), F32),
            ((HALF // quarters,), F32),
            ((quarter,), F32),
            ((2 * D // quarters, D), F32),
            ((quarter,), F32),
        ],
        "kvv",
        [((count,) + late_part.shape, BF16)],
        megas=24,
        aliases={0: 7},
    )(half_up, *late_parts)
    return (
        out_rows[None],
        grad_frames[None],
        *late[:4],
        grad_qkv,
        *late[4:6],
        grad_pos,
        *late[6:13],
        grad_down,
        *late[13:],
    )


def per_device(*operands):
    fits = (
        lax.axis_size("tm") == HEADS
        and lax.axis_size("stream") * LANES == D
        and operands[0].shape[1] == BLOCK
    )
    return head_device(*operands) if fits else frame_device(*operands)


def solution(mesh):
    return jax.shard_map(
        per_device,
        mesh=mesh,
        in_specs=(
            P("stream", "tm", None),
            P("stream", None),
            P("stream", "tm", None),
            P(),
            P(),
            P(),
            P(),
            P(),
            P(),
            P(),
            P(),
            P(),
            P(),
            P(),
            P(),
            P(),
            P(),
            P(),
            P(),
            P(),
            P(),
            P(),
        ),
        out_specs=(
            P("stream", "tm", None),
            P("stream", "tm", None),
            P("stream"),
            P("stream"),
            P("stream"),
            P("stream"),
            P("stream", None),
            P("stream"),
            P("stream"),
            P("stream", None),
            P("stream", None),
            P("stream", None),
            P("stream"),
            P("stream"),
            P("stream"),
            P(None, "stream"),
            P("stream"),
            P("stream", None),
            P("stream"),
            P("stream", None),
            P("stream"),
        ),
        check_vma=False,
    )
```

```python
import math

import jax
import jax.numpy as jnp
from jax import lax
from jax.experimental import pallas as pl
from jax.experimental.pallas import tpu as pltpu
from jax.sharding import PartitionSpec as P

D = 512
HEADS = 8
HEAD = 64
KERNEL = 31
ITEMS = 5
HALF = 1536


EPS = 1e-05
MASKED = -1e30


def extended(block, sides, width):
    for axis, dim in sides:
        count = lax.axis_size(axis)
        forward = [(i, i + 1) for i in range(count - 1)]
        backward = [(target, source) for source, target in forward]
        low = lax.ppermute(
            lax.slice_in_dim(block, block.shape[dim] - width, None, axis=dim), axis, forward
        )
        high = lax.ppermute(lax.slice_in_dim(block, 0, width, axis=dim), axis, backward)
        block = jnp.concatenate([low, block, high], axis=dim)
    return block


def norm_rows(inputs, scale_row, shift_row):
    row_mean = jnp.mean(inputs, axis=-1, keepdims=True)
    centred = inputs - row_mean
    spread = jnp.mean(centred * centred, axis=-1, keepdims=True)
    return centred * lax.rsqrt(spread + EPS) * scale_row + shift_row


def gelu_exact(inputs):
    return jax.nn.gelu(inputs, approximate=False)


def frame_info(lengths, offset, extent):
    item_ends = jnp.cumsum(lengths)
    first_table = jnp.concatenate([item_ends - lengths, item_ends[-1:]])
    frame_index = offset + jnp.arange(extent, dtype=jnp.int32)
    item_of = jnp.sum((frame_index[:, None] >= item_ends[None, :]).astype(jnp.int32), axis=1)
    labels = jnp.arange(ITEMS + 1, dtype=jnp.int32)
    first_frame = jnp.sum(
        jnp.where(item_of[:, None] == labels[None, :], first_table[None, :], 0), axis=1
    )
    return (frame_index, item_of, frame_index - first_frame)


def angles(place_in):
    frequency = jnp.exp(jnp.arange(D // 2, dtype=jnp.float32) * (-2.0 * math.log(10000.0) / D))
    phase_angle = place_in.astype(jnp.float32)[:, None] * frequency[None, :]
    return (jnp.sin(phase_angle), jnp.cos(phase_angle))


def rel_query(projected, sine_rows, cosine_rows):
    half_size = projected.shape[-1] // 2
    first_half = projected[..., :half_size]
    second_half = projected[..., half_size:]
    sine_wide = sine_rows[:, None, :]
    cosine_wide = cosine_rows[:, None, :]
    return jnp.concatenate(
        [
            first_half * sine_wide + second_half * cosine_wide,
            second_half * sine_wide - first_half * cosine_wide,
        ],
        axis=-1,
    )


def step_size(extent):
    return math.gcd(extent, 512)


def score_block(q_content, q_rel, query_item, query_frame, key_block, key_start, lengths):
    extent = key_block.shape[0]
    key_frame, key_item, key_place = frame_info(lengths, key_start, extent)
    sine_rows, cosine_rows = angles(key_place)
    k_rel = jnp.concatenate([cosine_rows, sine_rows], axis=1).astype(jnp.bfloat16)
    raw_scores = jnp.einsum(
        "qhe,khe->hqk",
        q_content,
        key_block.reshape(extent, HEADS, HEAD),
        preferred_element_type=jnp.float32,
    )
    raw_scores = raw_scores + jnp.einsum(
        "qhc,kc->hqk", q_rel, k_rel, preferred_element_type=jnp.float32
    )
    allowed = (query_item[:, None] == key_item[None, :]) & (
        (query_item[:, None] < ITEMS) | (query_frame[:, None] == key_frame[None, :])
    )
    return (raw_scores, allowed, k_rel)


def block_grads(
    q_content,
    q_rel,
    query_item,
    query_frame,
    grad_out,
    log_total,
    delta_rows,
    key_block,
    value_block,
    key_start,
    lengths,
):
    extent = key_block.shape[0]
    raw_scores, allowed, k_rel = score_block(
        q_content, q_rel, query_item, query_frame, key_block, key_start, lengths
    )
    prob_rows = jnp.where(allowed[None], jnp.exp(raw_scores * 0.125 - log_total[:, :, None]), 0.0)
    grad_prob = jnp.einsum(
        "qhe,khe->hqk",
        grad_out,
        value_block.reshape(extent, HEADS, HEAD),
        preferred_element_type=jnp.float32,
    )
    grad_raw = (prob_rows * (grad_prob - delta_rows[:, :, None]) * 0.125).astype(jnp.bfloat16)
    return (prob_rows.astype(jnp.bfloat16), grad_raw, k_rel)


def frame_device(
    frames,
    lengths,
    cotangent,
    ln_attn_gain,
    ln_attn_bias,
    ln_mlp_gain,
    ln_mlp_bias,
    qkv_weight,
    content_bias,
    position_bias,
    pos_weight,
    out_weight,
    up_weight,
    up_bias,
    gate_norm_gain,
    gate_norm_bias,
    conv_kernel,
    conv_bias,
    down_weight,
    down_bias,
    merge_weight,
    merge_bias,
):
    row_count = frames.shape[1]
    cycle_size = lax.axis_size("tm")
    offset = lax.axis_index("tm") * row_count
    stream_lengths = lengths[0]
    inputs = frames[0].astype(jnp.float32)
    frame_index, item_of, place_in = frame_info(stream_lengths, offset, row_count)
    sine_rows, cosine_rows = angles(place_in)
    attn_norm, attn_pull = jax.vjp(
        norm_rows, inputs, ln_attn_gain.astype(jnp.float32), ln_attn_bias.astype(jnp.float32)
    )
    mlp_norm, mlp_pull = jax.vjp(
        norm_rows, inputs, ln_mlp_gain.astype(jnp.float32), ln_mlp_bias.astype(jnp.float32)
    )
    attn_norm_low = attn_norm.astype(jnp.bfloat16)
    mlp_norm_low = mlp_norm.astype(jnp.bfloat16)
    qkv_rows = jnp.dot(attn_norm_low, qkv_weight, preferred_element_type=jnp.float32)
    query_rows = qkv_rows[:, :D]
    key_rows = qkv_rows[:, D : 2 * D].astype(jnp.bfloat16)
    value_rows = qkv_rows[:, 2 * D :].astype(jnp.bfloat16)
    q_content = (query_rows + content_bias.astype(jnp.float32)).astype(jnp.bfloat16)
    q_position = (query_rows + position_bias.astype(jnp.float32)).astype(jnp.bfloat16)
    content_heads = q_content.reshape(row_count, HEADS, HEAD)
    position_heads = q_position.reshape(row_count, HEADS, HEAD)
    pos_heads = pos_weight.reshape(D, HEADS, HEAD)
    projected = jnp.einsum(
        "the,che->thc", position_heads, pos_heads, preferred_element_type=jnp.float32
    )
    q_rel = rel_query(projected, sine_rows, cosine_rows).astype(jnp.bfloat16)
    start_state = (
        jnp.full((HEADS, row_count), MASKED, jnp.float32),
        jnp.zeros((HEADS, row_count), jnp.float32),
        jnp.zeros((HEADS, row_count, HEAD), jnp.float32),
    )
    fold_state = start_state
    key_piece = lax.all_gather(key_rows, "tm", axis=0, tiled=True)
    value_piece = lax.all_gather(value_rows, "tm", axis=0, tiled=True)
    extent = key_piece.shape[0]
    step_rows = step_size(extent)

    def forward_one_step(inner_state, step_index):
        row_top, row_total, row_acc = inner_state
        key_block = lax.dynamic_slice_in_dim(key_piece, step_index * step_rows, step_rows, 0)
        value_block = lax.dynamic_slice_in_dim(value_piece, step_index * step_rows, step_rows, 0)
        raw_scores, allowed, k_rel = score_block(
            content_heads,
            q_rel,
            item_of,
            frame_index,
            key_block,
            step_index * step_rows,
            stream_lengths,
        )
        scaled = jnp.where(allowed[None], raw_scores * 0.125, MASKED)
        new_top = jnp.maximum(row_top, jnp.max(scaled, axis=2))
        weight = jnp.where(allowed[None], jnp.exp(scaled - new_top[:, :, None]), 0.0)
        factor = jnp.exp(row_top - new_top)
        row_total = row_total * factor + jnp.sum(weight, axis=2)
        row_acc = row_acc * factor[:, :, None] + jnp.einsum(
            "hqk,khe->hqe",
            weight.astype(jnp.bfloat16),
            value_block.reshape(step_rows, HEADS, HEAD),
            preferred_element_type=jnp.float32,
        )
        return ((new_top, row_total, row_acc), None)

    fold_state, unused = lax.scan(
        forward_one_step, fold_state, jnp.arange(extent // step_rows, dtype=jnp.int32)
    )
    row_top, row_total, row_acc = fold_state
    attn_heads = row_acc / row_total[:, :, None]
    log_total = row_top + jnp.log(row_total)
    attn_low = jnp.transpose(attn_heads, (1, 0, 2)).reshape(row_count, D).astype(jnp.bfloat16)
    branch_attn = jnp.dot(attn_low, out_weight, preferred_element_type=jnp.float32).astype(
        jnp.bfloat16
    )
    hidden_pre = jnp.dot(
        mlp_norm_low, up_weight, preferred_element_type=jnp.float32
    ) + up_bias.astype(jnp.float32)
    hidden, gelu_pull = jax.vjp(gelu_exact, hidden_pre)
    gate_half = hidden[:, :HALF]
    conv_norm, conv_pull = jax.vjp(
        norm_rows,
        hidden[:, HALF:],
        gate_norm_gain.astype(jnp.float32),
        gate_norm_bias.astype(jnp.float32),
    )
    conv_in = conv_norm.astype(jnp.bfloat16)
    half_width = KERNEL // 2
    conv_wide = extended(conv_in, (("tm", 0),), half_width)
    wide_frame, wide_item, wide_place = frame_info(
        stream_lengths, offset - half_width, row_count + 2 * half_width
    )
    kernel_rows = conv_kernel.astype(jnp.float32)
    conv_out = conv_bias.astype(jnp.float32) + jnp.zeros_like(gate_half)
    for tap_index in range(KERNEL):
        same_item = (wide_item[tap_index : tap_index + row_count] == item_of)[:, None]
        conv_out = (
            conv_out
            + jnp.where(
                same_item, conv_wide[tap_index : tap_index + row_count].astype(jnp.float32), 0.0
            )
            * kernel_rows[tap_index]
        )
    gated_low = (gate_half * conv_out).astype(jnp.bfloat16)
    branch_mlp = (
        jnp.dot(gated_low, down_weight, preferred_element_type=jnp.float32)
        + down_bias.astype(jnp.float32)
    ).astype(jnp.bfloat16)
    joined = jnp.concatenate([branch_attn, branch_mlp], axis=1)
    result = (
        inputs
        + jnp.dot(joined, merge_weight, preferred_element_type=jnp.float32)
        + merge_bias.astype(jnp.float32)
    )
    out_rows = result.astype(jnp.bfloat16)[None]
    grad_low = cotangent[0]
    grad_rows = grad_low.astype(jnp.float32)
    grad_merge_bias = jnp.sum(grad_rows, axis=0)
    grad_merge_weight = jnp.einsum(
        "tc,td->cd", joined, grad_low, preferred_element_type=jnp.float32
    )
    grad_joined = jnp.einsum(
        "td,cd->tc", grad_low, merge_weight, preferred_element_type=jnp.float32
    )
    grad_attn_branch = grad_joined[:, :D].astype(jnp.bfloat16)
    grad_mlp_branch = grad_joined[:, D:].astype(jnp.bfloat16)
    grad_down_weight = jnp.einsum(
        "tc,td->cd", gated_low, grad_mlp_branch, preferred_element_type=jnp.float32
    )
    grad_down_bias = jnp.sum(grad_mlp_branch.astype(jnp.float32), axis=0)
    grad_gated = jnp.einsum(
        "td,cd->tc", grad_mlp_branch, down_weight, preferred_element_type=jnp.float32
    )
    grad_gate_half = grad_gated * conv_out
    grad_conv_out = (grad_gated * gate_half).astype(jnp.bfloat16)
    grad_conv_rows = grad_conv_out.astype(jnp.float32)
    grad_conv_bias = jnp.sum(grad_conv_rows, axis=0)
    grad_wide = extended(grad_conv_out, (("tm", 0),), half_width)
    kernel_list = []
    grad_conv_in = jnp.zeros_like(grad_conv_rows)
    for tap_index in range(KERNEL):
        same_item = (wide_item[tap_index : tap_index + row_count] == item_of)[:, None]
        kernel_list.append(
            jnp.sum(
                jnp.where(
                    same_item, conv_wide[tap_index : tap_index + row_count].astype(jnp.float32), 0.0
                )
                * grad_conv_rows,
                axis=0,
            )
        )
        back_start = 2 * half_width - tap_index
        back_item = (wide_item[back_start : back_start + row_count] == item_of)[:, None]
        grad_conv_in = (
            grad_conv_in
            + jnp.where(
                back_item, grad_wide[back_start : back_start + row_count].astype(jnp.float32), 0.0
            )
            * kernel_rows[tap_index]
        )
    grad_conv_kernel = jnp.stack(kernel_list)
    grad_second, grad_gate_norm_gain, grad_gate_norm_bias = conv_pull(grad_conv_in)
    (grad_pre_rows,) = gelu_pull(jnp.concatenate([grad_gate_half, grad_second], axis=1))
    grad_pre = grad_pre_rows.astype(jnp.bfloat16)
    grad_up_bias = jnp.sum(grad_pre.astype(jnp.float32), axis=0)
    grad_up_weight = jnp.einsum(
        "tc,tf->cf", mlp_norm_low, grad_pre, preferred_element_type=jnp.float32
    )
    grad_mlp_norm = jnp.einsum("tf,cf->tc", grad_pre, up_weight, preferred_element_type=jnp.float32)
    grad_out_weight = jnp.einsum(
        "tc,td->cd", attn_low, grad_attn_branch, preferred_element_type=jnp.float32
    )
    grad_attn_low = jnp.einsum(
        "td,cd->tc", grad_attn_branch, out_weight, preferred_element_type=jnp.float32
    ).astype(jnp.bfloat16)
    grad_out_heads = grad_attn_low.reshape(row_count, HEADS, HEAD)
    delta_rows = jnp.sum(
        jnp.transpose(grad_out_heads.astype(jnp.float32), (1, 0, 2)) * attn_heads, axis=2
    )
    total_frames = row_count * cycle_size
    back_start_state = (
        jnp.zeros((row_count, HEADS, HEAD), jnp.float32),
        jnp.zeros((row_count, HEADS, D), jnp.float32),
        jnp.zeros((total_frames, D), jnp.float32),
        jnp.zeros((total_frames, D), jnp.float32),
    )
    back_key_piece = lax.all_gather(key_rows, "tm", axis=0, tiled=True)
    back_value_piece = lax.all_gather(value_rows, "tm", axis=0, tiled=True)
    extent = back_key_piece.shape[0]
    back_step_rows = step_size(extent)

    def back_one_step(inner_state, step_index):
        grad_content, grad_rel = inner_state
        key_block = lax.dynamic_slice_in_dim(
            back_key_piece, step_index * back_step_rows, back_step_rows, 0
        )
        value_block = lax.dynamic_slice_in_dim(
            back_value_piece, step_index * back_step_rows, back_step_rows, 0
        )
        prob_low, grad_raw, k_rel = block_grads(
            content_heads,
            q_rel,
            item_of,
            frame_index,
            grad_out_heads,
            log_total,
            delta_rows,
            key_block,
            value_block,
            step_index * back_step_rows,
            stream_lengths,
        )
        grad_content = grad_content + jnp.einsum(
            "hqk,khe->qhe",
            grad_raw,
            key_block.reshape(back_step_rows, HEADS, HEAD),
            preferred_element_type=jnp.float32,
        )
        grad_rel = grad_rel + jnp.einsum(
            "hqk,kc->qhc", grad_raw, k_rel, preferred_element_type=jnp.float32
        )
        key_part = jnp.einsum(
            "hqk,qhe->khe", grad_raw, content_heads, preferred_element_type=jnp.float32
        ).reshape(back_step_rows, D)
        value_part = jnp.einsum(
            "hqk,qhe->khe", prob_low, grad_out_heads, preferred_element_type=jnp.float32
        ).reshape(back_step_rows, D)
        return ((grad_content, grad_rel), (key_part, value_part))

    inner_state, block_parts = lax.scan(
        back_one_step,
        (back_start_state[0], back_start_state[1]),
        jnp.arange(extent // back_step_rows, dtype=jnp.int32),
    )
    key_all = block_parts[0].reshape(extent, D)
    value_all = block_parts[1].reshape(extent, D)
    grad_content, grad_rel, key_all, value_all = (
        inner_state[0],
        inner_state[1],
        key_all,
        value_all,
    )
    grad_keys, grad_values = (
        lax.psum_scatter(key_all, "tm", scatter_dimension=0, tiled=True),
        lax.psum_scatter(value_all, "tm", scatter_dimension=0, tiled=True),
    )
    half_size = D // 2
    rel_first = grad_rel[..., :half_size]
    rel_second = grad_rel[..., half_size:]
    sine_wide = sine_rows[:, None, :]
    cosine_wide = cosine_rows[:, None, :]
    grad_projected = jnp.concatenate(
        [
            rel_first * sine_wide - rel_second * cosine_wide,
            rel_first * cosine_wide + rel_second * sine_wide,
        ],
        axis=-1,
    ).astype(jnp.bfloat16)
    grad_pos_weight = jnp.einsum(
        "thc,the->che", grad_projected, position_heads, preferred_element_type=jnp.float32
    ).reshape(D, D)
    grad_q_position = jnp.einsum(
        "thc,che->the", grad_projected, pos_heads, preferred_element_type=jnp.float32
    )
    grad_content_bias = jnp.sum(grad_content, axis=0).reshape(D)
    grad_position_bias = jnp.sum(grad_q_position, axis=0).reshape(D)
    grad_query = (grad_content + grad_q_position).reshape(row_count, D).astype(jnp.bfloat16)
    grad_qkv = jnp.concatenate(
        [grad_query, grad_keys.astype(jnp.bfloat16), grad_values.astype(jnp.bfloat16)], axis=1
    )
    grad_qkv_weight = jnp.einsum(
        "tc,tf->cf", attn_norm_low, grad_qkv, preferred_element_type=jnp.float32
    )
    grad_attn_norm = jnp.einsum(
        "tf,cf->tc", grad_qkv, qkv_weight, preferred_element_type=jnp.float32
    )
    grad_from_attn, grad_ln_attn_gain, grad_ln_attn_bias = attn_pull(grad_attn_norm)
    grad_from_mlp, grad_ln_mlp_gain, grad_ln_mlp_bias = mlp_pull(grad_mlp_norm)
    grad_inputs = grad_rows + grad_from_attn + grad_from_mlp
    weight_grads = (
        grad_ln_attn_gain,
        grad_ln_attn_bias,
        grad_ln_mlp_gain,
        grad_ln_mlp_bias,
        grad_qkv_weight,
        grad_content_bias,
        grad_position_bias,
        grad_pos_weight,
        grad_out_weight,
        grad_up_weight,
        grad_up_bias,
        grad_gate_norm_gain,
        grad_gate_norm_bias,
        grad_conv_kernel,
        grad_conv_bias,
        grad_down_weight,
        grad_down_bias,
        grad_merge_weight,
        grad_merge_bias,
    )
    summed = lax.psum(
        (
            weight_grads[0],
            weight_grads[1],
            weight_grads[2],
            weight_grads[3],
            weight_grads[4],
            weight_grads[5],
            weight_grads[6],
            weight_grads[7],
            weight_grads[8],
            weight_grads[9],
            weight_grads[10],
            weight_grads[11],
            weight_grads[12],
            weight_grads[13],
            weight_grads[14],
            weight_grads[15],
            weight_grads[16],
            weight_grads[17],
            weight_grads[18],
        ),
        "tm",
    )
    shares = (
        lax.psum_scatter(
            summed[0].astype(jnp.bfloat16), "stream", scatter_dimension=0, tiled=True
        ).astype(jnp.float32),
        lax.psum_scatter(
            summed[1].astype(jnp.bfloat16), "stream", scatter_dimension=0, tiled=True
        ).astype(jnp.float32),
        lax.psum_scatter(
            summed[2].astype(jnp.bfloat16), "stream", scatter_dimension=0, tiled=True
        ).astype(jnp.float32),
        lax.psum_scatter(
            summed[3].astype(jnp.bfloat16), "stream", scatter_dimension=0, tiled=True
        ).astype(jnp.float32),
        lax.psum_scatter(
            summed[4].astype(jnp.bfloat16), "stream", scatter_dimension=0, tiled=True
        ).astype(jnp.float32),
        lax.psum_scatter(
            summed[5].astype(jnp.bfloat16), "stream", scatter_dimension=0, tiled=True
        ).astype(jnp.float32),
        lax.psum_scatter(
            summed[6].astype(jnp.bfloat16), "stream", scatter_dimension=0, tiled=True
        ).astype(jnp.float32),
        lax.psum_scatter(
            summed[7].astype(jnp.bfloat16), "stream", scatter_dimension=0, tiled=True
        ).astype(jnp.float32),
        lax.psum_scatter(
            summed[8].astype(jnp.bfloat16), "stream", scatter_dimension=0, tiled=True
        ).astype(jnp.float32),
        lax.psum_scatter(
            summed[9].astype(jnp.bfloat16), "stream", scatter_dimension=0, tiled=True
        ).astype(jnp.float32),
        lax.psum_scatter(
            summed[10].astype(jnp.bfloat16), "stream", scatter_dimension=0, tiled=True
        ).astype(jnp.float32),
        lax.psum_scatter(
            summed[11].astype(jnp.bfloat16), "stream", scatter_dimension=0, tiled=True
        ).astype(jnp.float32),
        lax.psum_scatter(
            summed[12].astype(jnp.bfloat16), "stream", scatter_dimension=0, tiled=True
        ).astype(jnp.float32),
        lax.psum_scatter(
            summed[13].astype(jnp.bfloat16), "stream", scatter_dimension=1, tiled=True
        ).astype(jnp.float32),
        lax.psum_scatter(
            summed[14].astype(jnp.bfloat16), "stream", scatter_dimension=0, tiled=True
        ).astype(jnp.float32),
        lax.psum_scatter(
            summed[15].astype(jnp.bfloat16), "stream", scatter_dimension=0, tiled=True
        ).astype(jnp.float32),
        lax.psum_scatter(
            summed[16].astype(jnp.bfloat16), "stream", scatter_dimension=0, tiled=True
        ).astype(jnp.float32),
        lax.psum_scatter(
            summed[17].astype(jnp.bfloat16), "stream", scatter_dimension=0, tiled=True
        ).astype(jnp.float32),
        lax.psum_scatter(
            summed[18].astype(jnp.bfloat16), "stream", scatter_dimension=0, tiled=True
        ).astype(jnp.float32),
    )
    return (out_rows, grad_inputs[None]) + tuple(shares)


LANES = 128
LOW = LANES // 2
BLOCK = 128
TALL = 256
WINDOW = 64
MARGIN = 16
BOUNDS = 16
MEGA = 1024 * 1024
F32 = jnp.float32
BF16 = jnp.bfloat16


def dot_nn(left, right):
    return jnp.dot(left, right, preferred_element_type=F32)


def dot_tn(left, right):
    return lax.dot_general(left, right, (((0,), (0,)), ((), ())), preferred_element_type=F32)


def flip(values):
    return jnp.transpose(values.astype(F32)).astype(BF16)


def rows_of(index, size, base=0):
    return pl.ds(pl.multiple_of(index * size, size) + base, size)


def line_of(ref):
    return ref[...].astype(F32).reshape(1, ref.shape[0])


def fold_rows(values):
    return jnp.sum(values.reshape(values.shape[0] // 8, 8, values.shape[1]), axis=0)


def one_row(values):
    return jnp.sum(values, axis=0, keepdims=True)


def turn(values):
    return pltpu.roll(values, LOW, 1)


def low_lanes(rows):
    return lax.broadcasted_iota(jnp.int32, (rows, LANES), 1) < LOW


def centre_rows(inputs):
    mean = jnp.mean(inputs, axis=-1, keepdims=True)
    centred = inputs - mean
    spread = jnp.mean(centred * centred, axis=-1, keepdims=True)
    return centred * lax.rsqrt(spread + EPS)


def gelu_parts(values):
    phi = 0.5 + 0.5 * lax.erf(values * math.sqrt(0.5))
    bell = jnp.exp(values * values * -0.5)
    return values * phi, phi + values * bell * (1.0 / math.sqrt(2.0 * math.pi))


class Part:
    def __init__(self, shape=None, pairs=None, refs=1, late=False):
        self.shape, self.pairs, self.refs, self.late = shape, pairs, refs, late

    def buffer(self, operand):
        return self.shape or operand.shape

    def copies(self, refs, buffer):
        return self.pairs(refs, buffer) if self.pairs else [(refs[0], buffer)]


def blocks_part(half, late=False):
    def pairs(refs, buffer):
        place = lax.axis_index("tm")
        return [
            (
                ref.at[:, pl.ds(half * D, D)],
                buffer.at[rows_of(lax.bitwise_xor(jnp.int32(apart), place), BLOCK)],
            )
            for apart, ref in enumerate(refs)
        ]

    return Part((HEADS * BLOCK, D), pairs, HEADS, late)


def rows_part(first, size, late=False):
    return Part((size, D), lambda refs, buffer: [(refs[0].at[pl.ds(first, size)], buffer)], late=late)


class Fetch:
    def __init__(self, pairs, buffer, sems, first):
        self.buffer, self.begun = buffer, False
        self.pending = [
            pltpu.make_async_copy(source, target, sems.at[first + index])
            for index, (source, target) in enumerate(pairs)
        ]

    def begin(self):
        if not self.begun:
            for copy in self.pending:
                copy.start()
        self.begun = True

    def __call__(self):
        self.begin()
        for copy in self.pending:
            copy.wait()
        self.pending = []
        return self.buffer


def begin(*fetches):
    for fetch in fetches:
        fetch.begin()


class Send:
    def __init__(self, buffer, target, sems):
        self.buffer, self.target, self.sems, self.copies = buffer, target, sems, []

    def go(self, *index):
        source, target = (self.buffer.at[index], self.target.at[index]) if index else (self.buffer, self.target)
        copy = pltpu.make_async_copy(source, target, self.sems[len(self.copies)])
        copy.start()
        self.copies.append(copy)

    def finish(self):
        if not self.copies:
            self.go()


SPACES = {"v": pltpu.VMEM, "s": pltpu.SMEM, "k": pl.ANY}


def kernel_call(body, out_shapes, plan, scratch=(), megas=58, bounds=False, aliases=None):
    def call(*operands):
        in_specs, buffers, at = [], [], 0
        for item in plan:
            if item == "f":
                in_specs.append(pl.BlockSpec(memory_space=pl.ANY))
                buffers.append(pltpu.VMEM(operands[at].shape, operands[at].dtype))
                at += 1
            elif isinstance(item, Part):
                in_specs += [pl.BlockSpec(memory_space=pl.ANY)] * item.refs
                buffers.append(pltpu.VMEM(item.buffer(operands[at]), operands[at].dtype))
                at += item.refs
            else:
                in_specs.append(pl.BlockSpec(memory_space=SPACES[item]))
                at += 1
        sent = [out for out in out_shapes if len(out) > 2]
        buffers += [pltpu.VMEM(out[3] if len(out) > 3 else out[0], out[1]) for out in sent]
        sem_count = 96
        extra = [pltpu.SMEM((BOUNDS,), jnp.int32)] if bounds else []

        def outer(*refs):
            inputs, rest = refs[: len(in_specs)], refs[len(in_specs) :]
            outputs, rest = rest[: len(out_shapes)], rest[len(out_shapes) :]
            held, rest = list(rest[: len(buffers)]), rest[len(buffers) :]
            sems, rest = rest[0], rest[1:]
            given, at, used = [], 0, 0
            for item in plan:
                if item == "f":
                    given.append(Fetch([(inputs[at], held[0])], held.pop(0), sems, used))
                    given[-1].begin()
                    used += 1
                    at += 1
                elif isinstance(item, Part):
                    buffer = held.pop(0)
                    pairs = item.copies(inputs[at : at + item.refs], buffer)
                    given.append(Fetch(pairs, buffer, sems, used))
                    if not item.late:
                        given[-1].begin()
                    used += len(pairs)
                    at += item.refs
                else:
                    given.append(inputs[at])
                    at += 1
            results = []
            for out, ref in zip(out_shapes, outputs):
                if len(out) > 2:
                    target = out[4](ref) if len(out) > 3 else ref
                    results.append(Send(held.pop(0), target, [sems.at[used + index] for index in range(4)]))
                    used += 4
                else:
                    results.append(ref)
            assert used <= sem_count
            given = [item() if kind == "f" else item for kind, item in zip(plan, given)]
            body(*given, *results, *rest)
            for item in given:
                if isinstance(item, Fetch):
                    item()
            sends = [item for item in results if isinstance(item, Send)]
            for item in sends:
                item.finish()
            for item in sends:
                for copy in item.copies:
                    copy.wait()

        return pl.pallas_call(
            outer,
            out_shape=[jax.ShapeDtypeStruct(out[0], out[1]) for out in out_shapes],
            in_specs=in_specs,
            out_specs=[pl.BlockSpec(memory_space=pl.ANY if len(out) > 2 else pltpu.VMEM) for out in out_shapes],
            scratch_shapes=buffers
            + [pltpu.SemaphoreType.DMA((sem_count,))]
            + [pltpu.VMEM(shape, kind) for shape, kind in scratch]
            + extra,
            input_output_aliases=aliases or {},
            compiler_params=pltpu.CompilerParams(vmem_limit_bytes=megas * MEGA),
            cost_estimate=pl.CostEstimate(flops=0, bytes_accessed=0, transcendentals=0),
        )(*operands)

    return call


def fill_bounds(lengths_ref, bounds_s, total):
    bounds_s[0] = jnp.int32(0)
    end = jnp.int32(0)
    for item in range(ITEMS):
        end = end + lengths_ref[0, item]
        bounds_s[item + 1] = end
    for item in range(ITEMS + 1, BOUNDS):
        bounds_s[item] = jnp.int32(total)


def select_kernel(
    up_ref,
    up_bias_ref,
    gain_ref,
    bias_ref,
    conv_bias_ref,
    taps_ref,
    qkv_ref,
    pos_ref,
    content_ref,
    position_ref,
    up_out,
    table_out,
    qkv_out,
    pos_out,
    bias_out,
):
    place = lax.axis_index("tm")
    quarters = lax.axis_size("stream")
    share = HALF // (quarters * lax.axis_size("tm"))
    lane = lax.broadcasted_iota(jnp.int32, (1, 2 * LANES), 1)
    channel = jnp.where(lane < LANES + LOW, lane, lane - LOW)
    group = jnp.zeros_like(channel)
    for quarter in range(1, quarters):
        group = group + (channel >= quarter * share).astype(jnp.int32)
    source = group * (HALF // quarters) + share * place + channel - group * share
    chosen = (lax.broadcasted_iota(jnp.int32, (HALF, 2 * LANES), 0) == source).astype(F32).astype(BF16)
    gate = dot_nn(up_ref[:, :HALF], chosen)
    conv = dot_nn(up_ref[:, HALF:], chosen)
    up_out[:, :LANES] = gate[:, :LANES].astype(BF16)
    up_out[:, LANES : 2 * LANES] = jnp.where(low_lanes(D), gate[:, LANES:], conv[:, LANES:]).astype(BF16)
    up_out[:, 2 * LANES :] = conv[:, :LANES].astype(BF16)
    up_bias = line_of(up_bias_ref)
    lines = jnp.concatenate(
        [
            up_bias[:, :HALF],
            up_bias[:, HALF:],
            line_of(gain_ref),
            line_of(bias_ref),
            line_of(conv_bias_ref),
            jnp.zeros((3, HALF), F32),
        ],
        axis=0,
    )
    lines = dot_nn(lines.astype(BF16), chosen)
    taps = dot_nn(taps_ref[...], chosen)
    for part in range(2):
        lanes = slice(part * LANES, (part + 1) * LANES)
        table_out[part, :8] = lines[:, lanes]
        table_out[part, 8 : 8 + KERNEL] = taps[:, lanes]
        table_out[part, 8 + KERNEL :] = jnp.zeros((1, LANES), F32)

    odd = lax.rem(place, 2) == 1

    def head_lanes(ref, base):
        at = pl.ds(pl.multiple_of(lax.div(place, 2) * LANES + base, LANES), LANES)
        values = ref[:, at].astype(F32)
        values = jnp.where(odd, turn(values), values)
        return jnp.where(low_lanes(values.shape[0]), values, 0.0)

    for part in range(3):
        qkv_out[:, part * LANES : (part + 1) * LANES] = head_lanes(qkv_ref, part * D).astype(BF16)
    pos_out[...] = head_lanes(pos_ref, 0).astype(BF16)
    bias_out[...] = jnp.zeros((8, LANES), F32)
    for line, ref in enumerate((content_ref, position_ref)):
        values = line_of(ref)
        picked = values[:, :LANES]
        for tile in range(1, D // LANES):
            picked = jnp.where(
                lax.div(place, 2) == tile, values[:, tile * LANES : (tile + 1) * LANES], picked
            )
        picked = jnp.where(odd, turn(picked), picked)
        bias_out[line : line + 1] = jnp.where(low_lanes(1), picked, 0.0)


def angle_rows(coarse_ref, fine_ref, block, rows):
    half = D // 2
    base = coarse_ref[pl.ds(block, 1)]
    base_sine, base_cosine = base[:, :half], base[:, half:]
    sine, cosine = fine_ref[rows, :half], fine_ref[rows, half:]
    return base_sine * cosine + base_cosine * sine, base_cosine * cosine - base_sine * sine


def item_codes(bounds_s, index):
    code = jnp.zeros_like(index)
    for item in range(1, ITEMS + 1):
        code = code + (index >= bounds_s[item]).astype(jnp.int32)
    return jnp.where(code < ITEMS, code, ITEMS + index)


def attend_kernel(
    lengths_ref,
    x_ref,
    attn_gain_ref,
    attn_bias_ref,
    mlp_gain_ref,
    mlp_bias_ref,
    qkv_ref,
    pos_ref,
    bias_ref,
    coarse_ref,
    fine_ref,
    up_ref,
    up_bias_ref,
    n_attn_out,
    n_mlp_out,
    hat_out,
    q_position_out,
    query_out,
    key_out,
    value_out,
    prob_out,
    attn_out,
    mean_out,
    rate_out,
    key_s,
    pos_s,
    bounds_s,
):
    frames = n_attn_out.buffer.shape[0]
    half = D // 2
    fill_bounds(lengths_ref, bounds_s, frames)
    attn_gain, attn_bias = line_of(attn_gain_ref), line_of(attn_bias_ref)
    mlp_gain, mlp_bias = line_of(mlp_gain_ref), line_of(mlp_bias_ref)
    content, position = bias_ref[0:1], bias_ref[1:2]
    pos_s[...] = flip(pos_ref[...])
    x_ref = x_ref()
    begin(up_ref)
    lane = lax.broadcasted_iota(jnp.int32, (1, LANES), 1)
    spare = ((lane == HEAD) | (lane == HEAD + 1)).astype(F32)

    @pl.loop(0, frames // TALL, unroll=4)
    def _(block):
        rows = rows_of(block, TALL)
        for part in range(TALL // 32):
            at = pl.ds(pl.multiple_of(block * TALL + part * 32, 32), 32)
            hat = centre_rows(x_ref[at].astype(F32))
            hat_out.buffer[at] = hat.astype(BF16)
            n_attn_out.buffer[at] = (hat * attn_gain + attn_bias).astype(BF16)
            n_mlp_out.buffer[at] = (hat * mlp_gain + mlp_bias).astype(BF16)
        parts = dot_nn(n_attn_out.buffer[rows], qkv_ref[...])
        query = parts[:, :LANES]
        query_out.buffer[rows, :LANES] = ((query + content).astype(BF16).astype(F32) * 0.125).astype(BF16)
        q_position = (query + position).astype(BF16)
        q_position_out.buffer[rows] = q_position
        key_out.buffer[rows, :LANES] = parts[:, LANES : 2 * LANES].astype(BF16)
        value_out.buffer[rows] = (parts[:, 2 * LANES :] + spare).astype(BF16)
        projected = dot_nn(q_position, pos_s[...])
        for part in range(TALL // 32):
            at = pl.ds(pl.multiple_of(block * TALL + part * 32, 32), 32)
            inner = part * 32 % BLOCK
            sine, cosine = angle_rows(
                coarse_ref, fine_ref, block * (TALL // BLOCK) + part * 32 // BLOCK, slice(inner, inner + 32)
            )
            first = projected[part * 32 : part * 32 + 32, :half]
            second = projected[part * 32 : part * 32 + 32, half:]
            query_out.buffer[at, LANES : LANES + half] = ((first * sine + second * cosine) * 0.125).astype(BF16)
            query_out.buffer[at, LANES + half :] = ((second * sine - first * cosine) * 0.125).astype(BF16)
            key_out.buffer[at, LANES : LANES + half] = cosine.astype(BF16)
            key_out.buffer[at, LANES + half :] = sine.astype(BF16)

    for out in (n_attn_out, n_mlp_out, hat_out, q_position_out, query_out, key_out, value_out):
        out.go()
    up_ref = up_ref()
    up_bias = line_of(up_bias_ref)[:, HALF:]
    @pl.loop(0, frames // TALL, unroll=2)
    def _(block):
        values = dot_nn(n_mlp_out.buffer[rows_of(block, TALL)], up_ref[...])
        for part in range(TALL // 16):
            pre = values[part * 16 : part * 16 + 16] + up_bias
            hidden = pre * (0.5 + 0.5 * lax.erf(pre * math.sqrt(0.5)))
            mean = jnp.mean(hidden, axis=-1, keepdims=True)
            centred = hidden - mean
            rate = lax.rsqrt(jnp.mean(centred * centred, axis=-1, keepdims=True) + EPS)
            at = pl.ds(pl.multiple_of(block * TALL + part * 16, 16), 16)
            mean_out.buffer[at] = jnp.broadcast_to(mean, (16, LANES))
            rate_out.buffer[at] = jnp.broadcast_to(rate, (16, LANES))

    mean_out.go()
    rate_out.go()
    key_code = item_codes(bounds_s, lax.broadcasted_iota(jnp.int32, (1, frames), 1))

    low = low_lanes(32)
    for block in range(frames // TALL):
        rows = pl.ds(block * TALL, TALL)
        key_s[:, rows] = flip(key_out.buffer[rows])
    for block in range(frames // TALL):
        rows = pl.ds(block * TALL, TALL)
        raw = dot_nn(query_out.buffer[rows], key_s[...])
        for part in range(TALL // 32):
            start = block * TALL + part * 32
            index = start + lax.broadcasted_iota(jnp.int32, (32, 1), 0)
            scaled = jnp.where(
                item_codes(bounds_s, index) == key_code, raw[part * 32 : part * 32 + 32], MASKED
            )
            weight = jnp.exp(scaled - jnp.max(scaled, axis=1, keepdims=True))
            prob_out.buffer[pl.ds(start, 32)] = weight.astype(BF16)
        prob_out.go(rows)
        attn = dot_nn(prob_out.buffer[rows], value_out.buffer[...])
        for part in range(TALL // 32):
            own = attn[part * 32 : part * 32 + 32]
            share = 1.0 / own[:, HEAD : HEAD + 1]
            attn_out.buffer[pl.ds(block * TALL + part * 32, 32)] = jnp.where(low, own * share, share)


def fill_margins(wide_s, frames):
    edge = jnp.zeros((MARGIN, LANES), F32)
    wide_s[:MARGIN] = edge
    wide_s[MARGIN + frames : 2 * MARGIN + frames] = edge
    base = frames + 3 * MARGIN
    after = base + frames // 2
    low = low_lanes(MARGIN)
    wide_s[base - MARGIN : base] = jnp.where(low, 0.0, turn(wide_s[after - MARGIN : after]))
    wide_s[after : after + MARGIN] = jnp.where(low, turn(wide_s[base : base + MARGIN]), 0.0)


def item_span(bounds_s, frame):
    begin, end = bounds_s[0], bounds_s[BOUNDS - 1]
    for item in range(1, ITEMS + 1):
        edge = bounds_s[item]
        begin = jnp.where(frame >= edge, edge, begin)
    for item in range(ITEMS, 0, -1):
        edge = bounds_s[item]
        end = jnp.where(frame < edge, edge, end)
    return begin, end


def is_whole(bounds_s, start):
    begin, end = item_span(bounds_s, start)
    reach = KERNEL // 2
    low = (begin == 0) | (begin <= start - reach)
    high = (end == bounds_s[BOUNDS - 1]) | (end >= start + WINDOW + reach)
    return low & high & (end >= start + WINDOW)


def tap_limits(bounds_s, start):
    frame = start + lax.broadcasted_iota(jnp.int32, (WINDOW, LANES), 0)
    begin, end = item_span(bounds_s, frame)
    return begin - frame, end - frame


def grouped(values):
    return values.reshape(WINDOW // 8, 8, LANES)


def triple_places(step, frames):
    half = frames // 2
    return (
        pl.multiple_of(step * WINDOW, 2 * MARGIN),
        pl.multiple_of(step * WINDOW + half, 2 * MARGIN),
        pl.multiple_of(step * WINDOW + frames + 2 * MARGIN, 2 * MARGIN),
    )


def over_windows(bounds_s, frames, body):
    half = frames // 2

    @pl.loop(0, half // WINDOW)
    def _(step):
        start = step * WINDOW
        whole = is_whole(bounds_s, start) & is_whole(bounds_s, start + half)

        @pl.when(whole)
        def _():
            body(step, None)

        @pl.when(jnp.logical_not(whole))
        def _():
            first, second = tap_limits(bounds_s, start), tap_limits(bounds_s, start + half)
            low = low_lanes(WINDOW)
            rest = [jnp.where(low, one, other) for one, other in zip(first, second)]
            body(step, (first, second, rest))


def tap_mask(tap, limits):
    shift = tap - KERNEL // 2
    return None if limits is None else (limits[0] <= shift) & (limits[1] > shift)


def tap_view(window_ref, tap, mask):
    view = window_ref[tap + 1 : tap + 1 + WINDOW]
    return grouped(view if mask is None else jnp.where(mask, view, 0.0))


def mlp_first_kernel(
    lengths_ref,
    n_ref,
    up_ref,
    table_ref,
    mean_ref,
    rate_ref,
    cot_ref,
    merge_ref,
    down_ref,
    attn_ref,
    mixed_out,
    gate_pre_out,
    grad_out,
    rate_out,
    hat_out,
    early_out,
    vectors_out,
    lines_out,
    hat_s,
    slope_s,
    gate_s,
    hidden_s,
    gate_slope_s,
    conv_s,
    grad_s,
    out_s,
    back_s,
    branch_s,
    mix_s,
    taps_s,
    turn_s,
    tap_sum_s,
    columns_s,
    forward_s,
    backward_s,
    merge_s,
    flip_s,
    bounds_s,
):
    place = lax.axis_index("tm")
    frames = mix_s.shape[0]
    half = frames // 2
    blocks = frames // BLOCK
    quarters, early_rows, _ = early_out.buffer.shape
    share = early_rows // 8
    channels = quarters * share
    fill_bounds(lengths_ref, bounds_s, frames)
    for part in range(2):
        for tap in range(KERNEL):
            line = jnp.broadcast_to(table_ref[part, 8 + tap : 9 + tap], (8, LANES))
            taps_s[part, tap] = line
            turn_s[part, KERNEL - 1 - tap] = line
    tap_sum_s[...] = jnp.zeros(tap_sum_s.shape, F32)
    main, rest = table_ref[0, :8], table_ref[1, :8]
    mixed_bias = jnp.where(low_lanes(1), rest[0:1], rest[1:2])
    low = low_lanes(64)
    gate_pre_ref = gate_pre_out.buffer
    n_ref = n_ref()
    mean_ref, rate_ref = mean_ref(), rate_ref()
    begin(cot_ref, merge_ref, down_ref, attn_ref)

    def stat_rows(rows):
        return mean_ref[rows], rate_ref[rows]

    def chunk(start, base=0):
        return pl.ds(pl.multiple_of(start, 64) + base, 64)

    def conv_part(hidden, mean, rate, lines, rows, to_rows):
        hat = (hidden - mean) * rate
        hat_s[rows] = hat
        hat_out.buffer[rows] = hat.astype(BF16)
        conv_s[to_rows] = (hat * lines[2:3] + lines[3:4]).astype(BF16).astype(F32)

    @pl.loop(0, half // TALL, unroll=2)
    def _(block):
        pre = [dot_nn(n_ref[rows_of(block, TALL, base)], up_ref[...]) for base in (0, half)]
        for part in range(TALL // 64):
            inner = slice(part * 64, part * 64 + 64)
            start = block * TALL + part * 64
            mixed = []
            for values, base in zip(pre, (0, half)):
                rows = chunk(start, base)
                gate, gate_slope = gelu_parts(values[inner, :LANES] + main[0:1])
                hidden_s[rows] = gate
                gate_slope_s[rows] = gate_slope
                hidden, slope = gelu_parts(values[inner, 2 * LANES :] + main[1:2])
                mean, rate = stat_rows(rows)
                slope_s[rows] = slope * rate
                conv_part(hidden, mean, rate, main, rows, chunk(start, base + MARGIN))
                mixed.append((*gelu_parts(values[inner, LANES : 2 * LANES] + mixed_bias), mean, rate))
            (low_hidden, low_slope, low_mean, low_rate), (high_hidden, high_slope, high_mean, high_rate) = mixed
            rows = chunk(start, frames)
            hidden_s[rows] = jnp.where(low, low_hidden, turn(high_hidden))
            gate_slope_s[rows] = jnp.where(low, low_slope, turn(high_slope))
            rate = jnp.where(low, low_rate, high_rate)
            slope_s[rows] = jnp.where(low, turn(low_slope), high_slope) * rate
            conv_part(
                jnp.where(low, turn(low_hidden), high_hidden),
                jnp.where(low, low_mean, high_mean),
                rate,
                rest,
                rows,
                chunk(start, frames + 3 * MARGIN),
            )

    hat_out.go()
    fill_margins(conv_s, frames)
    tall = WINDOW + 2 * MARGIN
    outs = (0, half, frames)

    def convolve(step, limits):
        for index, base in enumerate(triple_places(step, frames)):
            forward_s[index] = conv_s[pl.ds(base, tall)]
        for index in range(3):
            own = None if limits is None else limits[index]
            total = jnp.zeros((WINDOW // 8, 8, LANES), F32)
            for tap in range(KERNEL):
                mask = tap_mask(tap, own)
                total = total + tap_view(forward_s.at[index], tap, mask) * taps_s[index // 2, tap][None]
            lines = rest if index == 2 else main
            out_s[rows_of(step, WINDOW, outs[index])] = total.reshape(WINDOW, LANES) + lines[4:5]

    over_windows(bounds_s, frames, convolve)
    cot_ref = cot_ref()
    merge_ref = merge_ref()
    down_ref = down_ref()
    attn_ref = attn_ref()
    down_ref[channels:] = jnp.zeros((2 * LANES - channels, D), BF16)
    merge_s[...] = flip(merge_ref[...])
    flip_s[...] = flip(down_ref[...])
    zero = jnp.zeros((8, LANES), F32)

    def branch_part(grad_gated, rows, to_rows, sums):
        up_sum, conv_sum = sums
        gate, conv = hidden_s[rows], out_s[rows]
        gate_pre = (grad_gated * conv * gate_slope_s[rows]).astype(BF16)
        gate_pre_ref[rows] = gate_pre
        grad_conv = (grad_gated * gate).astype(BF16).astype(F32)
        grad_s[to_rows] = grad_conv
        gate_pre = gate_pre.astype(F32)
        return gate * conv, gate_pre, (up_sum + fold_rows(gate_pre), conv_sum + fold_rows(grad_conv))

    def branch_step(block, sums):
        main_sums, rest_sums = sums
        grads = []
        for base in (0, half):
            rows = rows_of(block, TALL, base)
            branch = dot_nn(cot_ref[rows], merge_s[...]).astype(BF16)
            branch_s[rows] = branch
            grads.append(dot_nn(branch, flip_s[...]))
        for part in range(TALL // 64):
            inner = slice(part * 64, part * 64 + 64)
            start = block * TALL + part * 64
            for values, base in zip(grads, (0, half)):
                rows = chunk(start, base)
                gated, gate_pre, main_sums = branch_part(
                    values[inner, :LANES], rows, chunk(start, base + MARGIN), main_sums
                )
                mix_s[rows, :LANES] = gated.astype(BF16)
                gate_s[rows, :LANES] = gate_pre.astype(BF16)
            grad = jnp.where(low, grads[0][inner, LANES:], turn(grads[1][inner, LANES:]))
            gated, gate_pre, rest_sums = branch_part(
                grad, chunk(start, frames), chunk(start, frames + 3 * MARGIN), rest_sums
            )
            low_rows, high_rows = chunk(start), chunk(start, half)
            gate_s[low_rows, LANES:] = gate_pre.astype(BF16)
            gate_s[high_rows, LANES:] = turn(gate_pre).astype(BF16)
            mix_s[low_rows, LANES:] = jnp.where(low, gated, turn(attn_ref[low_rows])).astype(BF16)
            mix_s[high_rows, LANES:] = jnp.where(low, turn(gated), turn(attn_ref[high_rows])).astype(BF16)
        return main_sums, rest_sums

    (main_up, main_conv), (rest_up, rest_conv) = lax.fori_loop(
        0, half // TALL, branch_step, ((zero, zero), (zero, zero)), unroll=2
    )
    gate_pre_out.go()
    fill_margins(grad_s, frames)
    own = rows_of(place, BLOCK)
    lines_out[0:1] = one_row(fold_rows(branch_s[own].astype(F32)))
    lines_out[1:2] = one_row(fold_rows(cot_ref[own].astype(F32)))
    lines_out[2:8] = jnp.zeros((6, D), F32)
    grad_down = dot_tn(mix_s[...], branch_s[...])
    grad_gate = dot_tn(gate_s[...], n_ref[...])
    for quarter in range(quarters):
        for tile in range(4):
            early_out.buffer[quarter, tile * share : (tile + 1) * share] = grad_down[
                quarter * share : (quarter + 1) * share, tile * LANES : (tile + 1) * LANES
            ].astype(BF16)
        early_out.buffer[quarter, 4 * share :] = grad_gate[
            :channels, quarter * LANES : (quarter + 1) * LANES
        ].astype(BF16)
    early_out.go()
    for block in range(blocks):
        mixed_out.buffer[block, :BLOCK] = mix_s[block * BLOCK : (block + 1) * BLOCK]
    mixed_out.go(slice(None), pl.ds(0, BLOCK))

    def differentiate(step, limits):
        for index, base in enumerate(triple_places(step, frames)):
            forward_s[index] = conv_s[pl.ds(base, tall)]
            backward_s[index] = grad_s[pl.ds(base, tall)]
        for index in range(3):
            own = None if limits is None else limits[index]
            total = jnp.zeros((WINDOW // 8, 8, LANES), F32)
            centre = grouped(backward_s[index, MARGIN : MARGIN + WINDOW])
            for tap in range(KERNEL):
                mask = tap_mask(tap, own)
                total = total + tap_view(backward_s.at[index], tap, mask) * turn_s[index // 2, tap][None]
                tap_sum_s[index // 2, tap] += jnp.sum(tap_view(forward_s.at[index], tap, mask) * centre, axis=0)
            back_s[rows_of(step, WINDOW, outs[index])] = total.reshape(WINDOW, LANES)

    over_windows(bounds_s, frames, differentiate)
    lane = lax.broadcasted_iota(jnp.int32, (64, LANES), 1)

    def norm_part(rows, lines, sums):
        gain_sum, bias_sum = sums
        back, hat, slope = back_s[rows], hat_s[rows], slope_s[rows]
        grad = back * lines[2:3]
        grad_out.buffer[rows] = (grad * slope).astype(BF16)
        rate_out.buffer[rows] = slope.astype(BF16)
        along = back * hat
        return grad, along * lines[2:3], (gain_sum + fold_rows(along), bias_sum + fold_rows(back))

    def norm_step(block, sums):
        main_sums, rest_sums = sums
        for part in range(TALL // 64):
            start = block * TALL + part * 64
            pairs = []
            for base in (0, half):
                plain, along, main_sums = norm_part(chunk(start, base), main, main_sums)
                pairs.append([plain, along])
            plain, along, rest_sums = norm_part(chunk(start, frames), rest, rest_sums)
            for item, values in enumerate((plain, along)):
                pairs[0][item] = pairs[0][item] + jnp.where(low, values, 0.0)
                pairs[1][item] = pairs[1][item] + jnp.where(low, 0.0, values)
            for (plain, along), base in zip(pairs, (0, half)):
                columns_s[chunk(start, base)] = jnp.where(
                    lane == 0,
                    jnp.sum(plain, axis=-1, keepdims=True),
                    jnp.where(lane == 1, jnp.sum(along, axis=-1, keepdims=True), 0.0),
                )
        return main_sums, rest_sums

    (main_gain, main_bias), (rest_gain, rest_bias) = lax.fori_loop(
        0, half // TALL, norm_step, ((zero, zero), (zero, zero)), unroll=2
    )
    grad_out.go()
    rate_out.go()
    totals = jnp.concatenate(
        [jnp.transpose(columns_s[block * BLOCK : (block + 1) * BLOCK])[:2] for block in range(blocks)], axis=0
    )
    high = totals.astype(BF16)
    low_part = (totals - high.astype(F32)).astype(BF16)
    for block in range(blocks):
        mixed_out.buffer[block, BLOCK:, :LANES] = high
        mixed_out.buffer[block, BLOCK:, LANES:] = low_part
    mixed_out.go(slice(None), pl.ds(BLOCK, 2 * blocks))

    def vectors(part, lines):
        taps = jnp.sum(tap_sum_s[part], axis=1)[:KERNEL]
        stacked = jnp.concatenate([taps] + [one_row(line) for line in lines], axis=0)
        if part:
            stacked = stacked + turn(stacked)
        return jnp.transpose(
            jnp.concatenate([stacked, jnp.zeros((LANES - stacked.shape[0], LANES), F32)], axis=0)
        )

    vectors_out[:LANES] = vectors(0, (main_conv, main_gain, main_bias, main_up))
    vectors_out[LANES:] = vectors(1, (rest_conv, rest_gain, rest_bias, rest_up))[: channels - LANES]


def attend_back_kernel(
    cot_ref,
    merge_ref,
    head_ref,
    attn_ref,
    value_ref,
    prob_ref,
    key_ref,
    coarse_ref,
    fine_ref,
    pos_ref,
    query_ref,
    n_ref,
    q_position_ref,
    qkv_ref,
    hat_ref,
    gain_ref,
    early_ref,
    branch_out,
    total_out,
    pack_0,
    pack_1,
    pack_2,
    pack_3,
    lines_out,
    grad_s,
    raw_s,
    projected_s,
    parts_s,
    grads_s,
    merge_s,
    head_s,
    value_s,
    qkv_s,
):
    place = lax.axis_index("tm")
    frames = raw_s.shape[0]
    blocks = frames // BLOCK
    half = D // 2
    zero = jnp.zeros((8, LANES), F32)
    cot_ref, merge_ref, head_ref, attn_ref = cot_ref(), merge_ref(), head_ref(), attn_ref()
    head_ref[HEAD:] = jnp.zeros((LANES - HEAD, D), BF16)
    begin(value_ref, prob_ref, key_ref, pos_ref)
    merge_s[...] = flip(merge_ref[...])
    head_s[...] = flip(head_ref[...])

    @pl.loop(0, frames // TALL, unroll=4)
    def _(block):
        rows = rows_of(block, TALL)
        branch = dot_nn(cot_ref[rows], merge_s[...]).astype(BF16)
        branch_out.buffer[rows] = branch
        grad = (dot_nn(branch, head_s[...]) * attn_ref[rows, HEAD : HEAD + 1]).astype(BF16).astype(F32)
        delta = jnp.sum(grad * attn_ref[rows], axis=1, keepdims=True)
        high = delta.astype(BF16).astype(F32)
        lane = lax.broadcasted_iota(jnp.int32, (TALL, LANES), 1)
        grad = jnp.where(lane == HEAD, -high, jnp.where(lane == HEAD + 1, high - delta, grad))
        grad_s[rows] = grad.astype(BF16)

    branch_out.go()
    value_ref, prob_ref = value_ref(), prob_ref()
    value_s[...] = flip(value_ref[...])
    key_ref, pos_ref = key_ref(), pos_ref()
    begin(query_ref, n_ref, q_position_ref, qkv_ref, hat_ref, early_ref)

    def score_step(block, sums):
        content_sum, position_sum = sums
        rows = rows_of(block, TALL)
        grad = grad_s[rows]
        score = dot_nn(grad, value_s[...])
        for part in range(TALL // 32):
            at = pl.ds(pl.multiple_of(block * TALL + part * 32, 32), 32)
            inner = slice(part * 32, part * 32 + 32)
            raw_s[at] = (prob_ref[at].astype(F32) * score[inner]).astype(BF16)
        query = dot_nn(raw_s[rows], key_ref[...]) * 0.125
        for part in range(TALL // 32):
            at = pl.ds(pl.multiple_of(block * TALL + part * 32, 32), 32)
            inner = part * 32 % BLOCK
            sine, cosine = angle_rows(
                coarse_ref, fine_ref, block * (TALL // BLOCK) + part * 32 // BLOCK, slice(inner, inner + 32)
            )
            inner = slice(part * 32, part * 32 + 32)
            first, second = query[inner, LANES : LANES + half], query[inner, LANES + half :]
            projected_s[at, :half] = (first * sine - second * cosine).astype(BF16)
            projected_s[at, half:] = (first * cosine + second * sine).astype(BF16)
        position = dot_nn(projected_s[rows], pos_ref[...])
        content = query[:, :LANES]
        parts_s[rows, :LANES] = (content + position).astype(BF16)
        return content_sum + fold_rows(content), position_sum + fold_rows(position)

    content_sum, position_sum = lax.fori_loop(0, frames // TALL, score_step, (zero, zero), unroll=4)
    query_ref, n_ref, q_position_ref = query_ref(), n_ref(), q_position_ref()
    qkv_ref, hat_ref = qkv_ref(), hat_ref()
    qkv_s[...] = flip(qkv_ref[...])
    grad_key = dot_tn(query_ref[...], raw_s[...])
    grad_value = dot_tn(grad_s[...], prob_ref[...])
    for block in range(blocks):
        at = slice(block * BLOCK, (block + 1) * BLOCK)
        parts_s[at, LANES : 2 * LANES] = jnp.transpose(grad_key[:, at]).astype(BF16)
        parts_s[at, 2 * LANES :] = jnp.transpose(grad_value[:, at]).astype(BF16)
    grads_s[:HEAD] = dot_tn(parts_s[:, :LANES], n_ref[...])[:HEAD]
    grads_s[HEAD : 2 * HEAD] = dot_nn(grad_key.astype(BF16), n_ref[...])[:HEAD]
    grads_s[2 * HEAD : 3 * HEAD] = dot_nn(grad_value.astype(BF16), n_ref[...])[:HEAD]
    grads_s[3 * HEAD :] = dot_tn(q_position_ref[...], projected_s[...])[:HEAD]
    stream = lax.axis_index("stream")
    early_ref = early_ref()
    for apart, pack_out in enumerate((pack_0, pack_1, pack_2, pack_3)):
        quarter = lax.bitwise_xor(stream, jnp.int32(apart))
        lanes = pl.ds(pl.multiple_of(quarter * LANES, LANES), LANES)
        pack_out.buffer[: 4 * HEAD] = grads_s[:, lanes].astype(BF16)
        pack_out.buffer[4 * HEAD :] = early_ref[quarter]
        pack_out.go()
    gain = line_of(gain_ref)
    wide_zero = jnp.zeros((8, D), F32)

    def norm_step(block, sums):
        gain_sum, bias_sum = sums
        grad = dot_nn(parts_s[rows_of(block, TALL)], qkv_s[...])
        for part in range(TALL // 32):
            at = pl.ds(pl.multiple_of(block * TALL + part * 32, 32), 32)
            own = grad[part * 32 : part * 32 + 32]
            total_out.buffer[at] = (own * gain).astype(BF16)
            gain_sum = gain_sum + fold_rows(own * hat_ref[at].astype(F32))
            bias_sum = bias_sum + fold_rows(own)
        return gain_sum, bias_sum

    gain_sum, bias_sum = lax.fori_loop(0, frames // TALL, norm_step, (wide_zero, wide_zero), unroll=4)
    lane = lax.broadcasted_iota(jnp.int32, (1, LANES), 1)

    def own_lanes(sums):
        line = one_row(sums)
        line = line + turn(line)
        tiles = [
            jnp.where(lax.div(tile * LANES + lane, HEAD) == place, line, 0.0) for tile in range(D // LANES)
        ]
        return jnp.concatenate(tiles, axis=1)

    lines_out[...] = jnp.concatenate(
        [
            one_row(gain_sum),
            one_row(bias_sum),
            own_lanes(content_sum),
            own_lanes(position_sum),
            jnp.zeros((4, D), F32),
        ],
        axis=0,
    )


def mlp_second_kernel(
    mixed_ref,
    gate_pre_ref,
    grad_ref,
    rate_ref,
    hat_ref,
    up_ref,
    norm_hat_ref,
    gain_ref,
    other_ref,
    pre_out,
    same_out,
    apart_out,
    lines_out,
    up_out,
    columns_s,
    flip_s,
):
    place = lax.axis_index("tm")
    pre_s = pre_out.buffer
    frames = pre_s.shape[0]
    half = frames // 2
    blocks = frames // BLOCK
    totals = jnp.zeros((2 * blocks, LANES), F32)
    mixed_ref = mixed_ref()
    for source in range(mixed_ref.shape[0]):
        both = mixed_ref[source].astype(F32)
        totals = totals + (both[:, :LANES] + both[:, LANES:])
    totals = totals * (1.0 / HALF)
    high = totals.astype(BF16)
    low_part = (totals - high.astype(F32)).astype(BF16)
    both = jnp.concatenate([high, low_part], axis=0)
    lane = lax.broadcasted_iota(jnp.int32, (4 * blocks, 2 * LANES), 1) // LANES
    line = lax.broadcasted_iota(jnp.int32, (4 * blocks, 2 * LANES), 0)
    for block in range(blocks):
        chosen = (lax.rem(line, 2 * blocks) == 2 * block + lane).astype(F32).astype(BF16)
        columns_s[block * BLOCK : (block + 1) * BLOCK] = dot_tn(both, chosen)
    gate_pre_ref, grad_ref, rate_ref, hat_ref = gate_pre_ref(), grad_ref(), rate_ref(), hat_ref()
    begin(up_ref, norm_hat_ref, other_ref)
    low = low_lanes(64)
    gain = line_of(gain_ref)

    def chunk(start, base=0):
        return pl.ds(pl.multiple_of(start, 64) + base, 64)

    def pre_part(rows, table, up_sum):
        plain, along = table
        hat, rate = hat_ref[rows].astype(F32), rate_ref[rows].astype(F32)
        pre = (grad_ref[rows].astype(F32) - rate * (plain + hat * along)).astype(BF16).astype(F32)
        return pre, up_sum + fold_rows(pre)

    def pre_step(block, sums):
        main_up, rest_up = sums
        for part in range(TALL // 64):
            start = block * TALL + part * 64
            tables = []
            for base in (0, half):
                rows = chunk(start, base)
                table = [columns_s[rows, item * LANES : (item + 1) * LANES] for item in range(2)]
                tables.append(table)
                pre, main_up = pre_part(rows, table, main_up)
                pre_s[rows, :LANES] = gate_pre_ref[rows]
                pre_s[rows, 2 * LANES :] = pre.astype(BF16)
            rows = chunk(start, frames)
            table = [jnp.where(low, one, other) for one, other in zip(*tables)]
            pre, rest_up = pre_part(rows, table, rest_up)
            gate_pre = gate_pre_ref[rows].astype(F32)
            pre_s[chunk(start), LANES : 2 * LANES] = jnp.where(low, gate_pre, turn(pre)).astype(BF16)
            pre_s[chunk(start, half), LANES : 2 * LANES] = jnp.where(low, turn(gate_pre), pre).astype(BF16)
        return main_up, rest_up

    zero = jnp.zeros((8, LANES), F32)
    main_up, rest_up = lax.fori_loop(0, half // TALL, pre_step, (zero, zero), unroll=2)
    pre_out.go()
    up_ref, norm_hat_ref, other_ref = up_ref(), norm_hat_ref(), other_ref()
    flip_s[...] = flip(up_ref[...])
    wide_zero = jnp.zeros((8, D), F32)

    def norm_step(step, sums):
        gain_sum, bias_sum = sums
        grads = dot_nn(pre_s[rows_of(step, TALL)], flip_s[...])
        for part in range(TALL // BLOCK):
            block = step * (TALL // BLOCK) + part
            rows = rows_of(block, BLOCK)
            grad = grads[part * BLOCK : (part + 1) * BLOCK]
            total = (grad * gain + other_ref[rows].astype(F32)).astype(BF16)
            apart = lax.bitwise_xor(block, place)

            @pl.when(lax.rem(apart, 2) == 0)
            def _(apart=apart, total=total):
                same_out.buffer[lax.div(apart, 2)] = total

            @pl.when(lax.rem(apart, 2) == 1)
            def _(apart=apart, total=total):
                apart_out.buffer[lax.div(apart, 2)] = total

            gain_sum = gain_sum + fold_rows(grad * norm_hat_ref[rows].astype(F32))
            bias_sum = bias_sum + fold_rows(grad)
        return gain_sum, bias_sum

    gain_sum, bias_sum = lax.fori_loop(0, frames // TALL, norm_step, (wide_zero, wide_zero), unroll=2)
    apart_out.go()
    same_out.go()
    lines_out[...] = jnp.concatenate([one_row(gain_sum), one_row(bias_sum), jnp.zeros((6, D), F32)], axis=0)
    rest_line = one_row(rest_up)
    up_out[:LANES] = jnp.transpose(jnp.broadcast_to(one_row(main_up), (LANES, LANES)))
    up_out[LANES:] = jnp.transpose(jnp.broadcast_to(rest_line + turn(rest_line), (LANES, LANES)))[:LOW]


def late_pack_kernel(
    pre_ref,
    n_ref,
    joined_ref,
    branch_ref,
    cot_ref,
    vectors_ref,
    up_columns_ref,
    first_lines_ref,
    head_lines_ref,
    own_lines_ref,
    pack_out,
):
    pack_ref = pack_out.buffer
    quarters = pack_ref.shape[0]
    channels = vectors_ref.shape[0]
    share = channels // quarters
    gate_at = KERNEL + 3
    lane = lax.broadcasted_iota(jnp.int32, (share, LANES), 1)
    lines = jnp.concatenate(
        [
            head_lines_ref[0:2],
            own_lines_ref[0:2],
            head_lines_ref[2:4],
            first_lines_ref[0:2],
            jnp.zeros((8, D), F32),
        ],
        axis=0,
    )
    for quarter in range(quarters):
        table = vectors_ref[quarter * share : (quarter + 1) * share]
        for other in range(2):
            at = slice((2 * (quarter % 2) + other) * share, (2 * (quarter % 2) + other + 1) * share)
            column = vectors_ref[at, gate_at : gate_at + 1] if quarter < quarters // 2 else up_columns_ref[at, 0:1]
            table = jnp.where(lane == gate_at + other, column, table)
        pack_ref[quarter, channels : channels + share] = table.astype(BF16)
        pack_ref[quarter, channels + share : channels + share + 16] = lines[
            :, quarter * LANES : (quarter + 1) * LANES
        ].astype(BF16)
    grad_up = dot_tn(pre_ref()[...], n_ref()[...])
    for quarter in range(quarters):
        lanes = slice(quarter * LANES, (quarter + 1) * LANES)
        pack_ref[quarter, :LANES] = grad_up[LANES:, lanes].astype(BF16)
        pack_ref[quarter, LANES:channels] = grad_up[LOW:LANES, lanes].astype(BF16)
    joined_ref, cot_ref, branch_ref = joined_ref(), cot_ref(), branch_ref()
    sources, _, rows = joined_ref.shape
    merge_rows = 2 * D // sources
    head_rows = D // sources
    grad_merge = jnp.zeros((merge_rows, D), F32)
    grad_head = jnp.zeros((head_rows, D), F32)
    for source in range(sources):
        at = slice(source * rows, (source + 1) * rows)
        joined = joined_ref[source]
        grad_merge = grad_merge + dot_nn(joined[:merge_rows], cot_ref[at])
        grad_head = grad_head + dot_nn(joined[merge_rows : merge_rows + head_rows], branch_ref[at])
    for quarter in range(quarters):
        base = channels + share + 16
        for grad in (grad_merge, grad_head):
            part = grad.shape[0] // quarters
            for tile in range(4):
                pack_ref[quarter, base : base + part] = grad[
                    quarter * part : (quarter + 1) * part, tile * LANES : (tile + 1) * LANES
                ].astype(BF16)
                base += part


def output_kernel(
    x_ref, mixed_ref, head_ref, down_ref, down_bias_ref, merge_ref, merge_bias_ref, out_ref, joined_out
):
    sources = mixed_ref.shape[0]
    rows = x_ref.shape[0]
    channels = HALF // sources
    share = channels // 4
    attn_parts = []
    branch_attn = jnp.zeros((rows, D), F32)
    branch_mlp = jnp.zeros((rows, D), F32)
    for source in range(sources):
        attn = turn(mixed_ref[source, :rows, LANES:].astype(F32))[:, :HEAD].astype(BF16)
        attn_parts.append(attn)
        branch_attn = branch_attn + dot_nn(attn, head_ref[source * HEAD : (source + 1) * HEAD])
        down = jnp.concatenate(
            [down_ref[(part * sources + source) * share : (part * sources + source + 1) * share] for part in range(4)],
            axis=0,
        )
        branch_mlp = branch_mlp + dot_nn(mixed_ref[source, :rows, :channels], down)
    joined = jnp.concatenate(
        [branch_attn.astype(BF16), (branch_mlp + line_of(down_bias_ref)).astype(BF16)], axis=1
    )
    result = x_ref[...].astype(F32) + dot_nn(joined, merge_ref[...]) + line_of(merge_bias_ref)
    out_ref[...] = result.astype(BF16)
    turned = jnp.transpose(joined.astype(F32))
    heads = jnp.transpose(jnp.concatenate(attn_parts, axis=1).astype(F32))
    merge_share = turned.shape[0] // (4 * sources)
    head_share = heads.shape[0] // (4 * sources)
    used = 4 * (merge_share + head_share)
    for target in range(sources):
        for part in range(4):
            at = (part * sources + target) * merge_share
            joined_out[target, part * merge_share : (part + 1) * merge_share] = turned[
                at : at + merge_share
            ].astype(BF16)
            at = (part * sources + target) * head_share
            to = 4 * merge_share + part * head_share
            joined_out[target, to : to + head_share] = heads[at : at + head_share].astype(BF16)
        joined_out[target, used:] = jnp.zeros((joined_out.shape[1] - used, rows), BF16)


def pair_kernel(same_ref, other_ref, *out_refs):
    for slot, out_ref in enumerate(out_refs):
        out_ref[...] = (same_ref[slot].astype(F32) + other_ref[slot].astype(F32)).astype(BF16)


def frames_kernel(x_ref, cot_ref, *refs):
    total_refs, out_ref = refs[:-1], refs[-1]
    for part in range(x_ref.shape[0] // 32):
        rows = slice(part * 32, part * 32 + 32)
        inputs = x_ref[rows].astype(F32)
        mean = jnp.mean(inputs, axis=-1, keepdims=True)
        centred = inputs - mean
        rate = lax.rsqrt(jnp.mean(centred * centred, axis=-1, keepdims=True) + EPS)
        hat = centred * rate
        grad = total_refs[0][rows].astype(F32)
        for total_ref in total_refs[1:]:
            grad = grad + total_ref[rows].astype(F32)
        plain = jnp.mean(grad, axis=-1, keepdims=True)
        along = jnp.mean(grad * hat, axis=-1, keepdims=True)
        out_ref[rows] = cot_ref[rows].astype(F32) + rate * (grad - plain - hat * along)


def add_kernel(*refs):
    out_ref = refs[-1]
    first = 0
    for at in range(0, len(refs) - 1, 4):
        total = refs[at][...].astype(F32)
        for ref in refs[at + 1 : at + 4]:
            total = total + ref[...].astype(F32)
        out_ref[first : first + total.shape[0]] = total.astype(BF16)
        first += total.shape[0]


def gather_parts(near_ref, far_ref, all_s):
    place = lax.axis_index("tm")
    for apart in range(all_s.shape[0]):
        part_ref = far_ref if apart % 2 else near_ref
        all_s[lax.bitwise_xor(jnp.int32(apart), place)] = part_ref[apart // 2]


def lines_from(all_s, base, size):
    return jnp.concatenate([all_s[source, base : base + size] for source in range(all_s.shape[0])], axis=0).astype(F32)


def add_streams_kernel(parts_ref, out_ref):
    total = parts_ref[0].astype(F32)
    for source in range(1, parts_ref.shape[0]):
        total = total + parts_ref[source].astype(F32)
    out_ref[...] = total.astype(BF16)


def early_kernel(near_ref, far_ref, qkv_out, pos_out, down_out, up_out, all_s):
    gather_parts(near_ref, far_ref, all_s)
    sources = all_s.shape[0]
    share = HALF // (4 * sources)
    for kind in range(4):
        lines = jnp.transpose(lines_from(all_s, kind * HEAD, HEAD))
        if kind < 3:
            qkv_out[:, kind * D : (kind + 1) * D] = lines
        else:
            pos_out[...] = lines
    base = 4 * HEAD
    for source in range(sources):
        for tile in range(4):
            down_out[source * share : (source + 1) * share, tile * LANES : (tile + 1) * LANES] = all_s[
                source, base + tile * share : base + (tile + 1) * share
            ].astype(F32)
    wide = sources * share
    for group in range(4):
        up_out.buffer[:, group * wide : (group + 1) * wide] = jnp.transpose(
            lines_from(all_s, base + 4 * share + group * share, share)
        )


def late_kernel(*refs):
    _, near_ref, far_ref = refs[:3]
    (
        attn_gain_out,
        attn_bias_out,
        mlp_gain_out,
        mlp_bias_out,
        content_out,
        position_out,
        outw_out,
        up_out,
        up_bias_out,
        gain_out,
        bias_out,
        taps_out,
        conv_bias_out,
        down_bias_out,
        merge_out,
        merge_bias_out,
        all_s,
    ) = refs[3:]
    gather_parts(near_ref, far_ref, all_s)
    sources = all_s.shape[0]
    channels = HALF // sources
    share = channels // 4
    base = 0
    for group in range(4):
        at = group * sources * share
        up_out.buffer[:, at : at + sources * share] = jnp.transpose(lines_from(all_s, base + group * share, share))
    up_out.go()
    table = jnp.transpose(lines_from(all_s, base + channels, share))
    taps_out[...] = table[:KERNEL]
    conv_bias_out[...] = table[KERNEL]
    gain_out[...] = table[KERNEL + 1]
    bias_out[...] = table[KERNEL + 2]
    wide = sources * share
    up_bias_out[:wide] = table[KERNEL + 3]
    up_bias_out[wide:] = table[KERNEL + 4]
    base = base + channels + share
    lines = all_s[0, base : base + 16].astype(F32)
    for source in range(1, sources):
        lines = lines + all_s[source, base : base + 16].astype(F32)
    outs = (attn_gain_out, attn_bias_out, mlp_gain_out, mlp_bias_out, content_out, position_out, down_bias_out, merge_bias_out)
    for line, out in enumerate(outs):
        out[...] = lines[line]
    base = base + 16
    merge_share = 2 * D // (4 * sources)
    head_share = D // (4 * sources)
    for source in range(sources):
        for tile in range(4):
            lanes = slice(tile * LANES, (tile + 1) * LANES)
            at = base + tile * merge_share
            merge_out[source * merge_share : (source + 1) * merge_share, lanes] = all_s[
                source, at : at + merge_share
            ].astype(F32)
            at = base + 4 * merge_share + tile * head_share
            outw_out[source * head_share : (source + 1) * head_share, lanes] = all_s[
                source, at : at + head_share
            ].astype(F32)


def moved(block, axis, bits):
    count = lax.axis_size(axis)
    return lax.ppermute(block, axis, [(index, index ^ bits) for index in range(count)])


def over_streams(packs):
    return [packs[0]] + [moved(packs[bits], "stream", bits) for bits in range(1, lax.axis_size("stream"))]


def near_blocks(block):
    return [block] + [moved(block, "tm", bits) for bits in range(2, lax.axis_size("tm"), 2)]


def far_blocks(near):
    far = [moved(part, "tm", 1) for part in near]
    return [part for pair in zip(near, far) for part in pair]


def far_stack(near):
    stack = jnp.stack(near)
    return stack, moved(stack, "tm", 1)


def head_device(
    frames,
    lengths,
    cotangent,
    ln_attn_gain,
    ln_attn_bias,
    ln_mlp_gain,
    ln_mlp_bias,
    qkv_weight,
    content_bias,
    position_bias,
    pos_weight,
    out_weight,
    up_weight,
    up_bias,
    gate_norm_gain,
    gate_norm_bias,
    conv_kernel,
    conv_bias,
    down_weight,
    down_bias,
    merge_weight,
    merge_bias,
):
    count = lax.axis_size("tm")
    quarters = lax.axis_size("stream")
    own = frames.shape[1]
    total = own * count
    folded = total + total // 2
    padded = folded + 4 * MARGIN
    share = HALF // (quarters * count)
    channels = HALF // count
    quarter = D // quarters
    own_frames = frames[0]
    own_cotangent = cotangent[0]

    whole, late = Part(), Part(late=True)
    near = near_blocks(jnp.concatenate([own_frames, own_cotangent], axis=1))
    up_own, table, qkv_own, pos_own, bias_own = kernel_call(
        select_kernel,
        [
            ((D, 3 * LANES), BF16),
            ((2, 8 + KERNEL + 1, LANES), F32),
            ((D, 3 * LANES), BF16),
            ((D, LANES), BF16),
            ((8, LANES), F32),
        ],
        10 * "v",
    )(
        up_weight,
        up_bias,
        gate_norm_gain,
        gate_norm_bias,
        conv_bias,
        conv_kernel,
        qkv_weight,
        pos_weight,
        content_bias,
        position_bias,
    )
    frequency = jnp.exp(jnp.arange(D // 2, dtype=F32) * (-2.0 * math.log(10000.0) / D))
    coarse = jnp.arange(0, total, BLOCK, dtype=F32)[:, None] * frequency[None]
    fine = jnp.arange(BLOCK, dtype=F32)[:, None] * frequency[None]
    coarse_table = jnp.concatenate([jnp.sin(coarse), jnp.cos(coarse)], axis=1)
    fine_table = jnp.concatenate([jnp.sin(fine), jnp.cos(fine)], axis=1)
    near, up_own, coarse_table, fine_table = lax.optimization_barrier((near, up_own, coarse_table, fine_table))
    blocks = far_blocks(near)

    n_attn, n_mlp, hat, q_position, query, key, value, prob, attn, mean, rate = kernel_call(
        attend_kernel,
        [
            ((total, D), BF16, 1),
            ((total, D), BF16, 1),
            ((total, D), BF16, 1),
            ((total, LANES), BF16, 1),
            ((total, LANES + D), BF16, 1),
            ((total, LANES + D), BF16, 1),
            ((total, LANES), BF16, 1),
            ((total, total), BF16, 1),
            ((total, LANES), F32, 1),
            ((total, LANES), F32, 1),
            ((total, LANES), F32, 1),
        ],
        [
            "s",
            blocks_part(0),
            *"vvvvvvvvv",
            Part((D, HALF), lambda refs, buffer: [(refs[0].at[:, pl.ds(HALF, HALF)], buffer)], late=True),
            "v",
        ],
        [((LANES + D, total), BF16), ((LANES, D), BF16)],
        bounds=True,
    )(
        lengths,
        *blocks,
        ln_attn_gain,
        ln_attn_bias,
        ln_mlp_gain,
        ln_mlp_bias,
        qkv_own,
        pos_own,
        bias_own,
        coarse_table,
        fine_table,
        up_weight,
        up_bias,
    )

    def own_down(refs, buffer):
        place = lax.axis_index("tm")
        stride = HALF // quarters
        return [
            (
                refs[0].at[pl.ds(pl.multiple_of(part * stride + share * place, 16), share)],
                buffer.at[pl.ds(part * share, share)],
            )
            for part in range(quarters)
        ]

    mixed, gate_pre, grad_y, slope, gate_hat, early_pack, vectors, first_lines = kernel_call(
        mlp_first_kernel,
        [
            ((count, own + 16, 2 * LANES), BF16, 1),
            ((folded, LANES), BF16, 1),
            ((folded, LANES), BF16, 1),
            ((folded, LANES), BF16, 1),
            ((folded, LANES), BF16, 1),
            ((quarters, 8 * share, LANES), BF16, 1),
            ((channels, LANES), F32),
            ((8, D), F32),
        ],
        [
            "s",
            whole,
            "v",
            "v",
            whole,
            whole,
            blocks_part(1, late=True),
            rows_part(D, D, late=True),
            Part((2 * LANES, D), own_down, late=True),
            Part(late=True),
        ],
        [
            ((folded, LANES), F32),
            ((folded, LANES), F32),
            ((total, 2 * LANES), BF16),
            ((folded, LANES), F32),
            ((folded, LANES), F32),
            ((padded, LANES), F32),
            ((padded, LANES), F32),
            ((folded, LANES), F32),
            ((folded, LANES), F32),
            ((total, D), BF16),
            ((total, 2 * LANES), BF16),
            ((2, 32, 8, LANES), F32),
            ((2, 32, 8, LANES), F32),
            ((2, 32, 8, LANES), F32),
            ((total, LANES), F32),
            ((3, WINDOW + 2 * MARGIN, LANES), F32),
            ((3, WINDOW + 2 * MARGIN, LANES), F32),
            ((D, D), BF16),
            ((D, 2 * LANES), BF16),
        ],
        bounds=True,
    )(lengths, n_mlp, up_own, table, mean, rate, *blocks, merge_weight, down_weight, attn)
    mixed_own = lax.all_to_all(mixed, "tm", 0, 0, tiled=True)

    def own_head(refs, buffer):
        at = pl.ds(pl.multiple_of(lax.axis_index("tm") * HEAD, HEAD), HEAD)
        return [(refs[0].at[at], buffer.at[pl.ds(0, HEAD)])]

    branch, from_attn, *head_packs, head_lines = kernel_call(
        attend_back_kernel,
        [
            ((total, D), BF16, 1),
            ((total, D), BF16, 1),
            *([((4 * HEAD + 8 * share, LANES), BF16, 1)] * quarters),
            ((8, D), F32),
        ],
        [
            blocks_part(1),
            rows_part(0, D),
            Part((LANES, D), own_head),
            whole,
            late,
            late,
            late,
            "v",
            "v",
            late,
            Part((total, LANES), lambda refs, buffer: [(refs[0].at[:, pl.ds(0, LANES)], buffer)], late=True),
            late,
            late,
            late,
            late,
            "v",
            late,
        ],
        [
            ((total, LANES), BF16),
            ((total, total), BF16),
            ((total, D), BF16),
            ((total, 3 * LANES), BF16),
            ((4 * HEAD, D), F32),
            ((D, D), BF16),
            ((D, LANES), BF16),
            ((LANES, total), BF16),
            ((3 * LANES, D), BF16),
        ],
    )(
        *blocks,
        merge_weight,
        out_weight,
        attn,
        value,
        prob,
        key,
        coarse_table,
        fine_table,
        pos_own,
        query,
        n_attn,
        q_position,
        qkv_own,
        hat,
        ln_attn_gain,
        early_pack,
    )
    head_parts = over_streams(head_packs)
    mixed_own, _ = lax.optimization_barrier((mixed_own, head_lines))
    out_rows, joined = kernel_call(
        output_kernel,
        [((own, D), BF16), ((count, 256, own), BF16)],
        "vvvvvvv",
        megas=24,
    )(own_frames, mixed_own, out_weight, down_weight, down_bias, merge_weight, merge_bias)
    joined_all = lax.all_to_all(joined, "tm", 0, 0, tiled=True)
    gate_pre, _ = lax.optimization_barrier((gate_pre, joined))
    late_rows = 5 * share + 16 + 3 * D // count
    pre, same, apart, own_lines, up_columns = kernel_call(
        mlp_second_kernel,
        [
            ((total, 3 * LANES), BF16, 1),
            ((count // 2, own, D), BF16, 1),
            ((count // 2, own, D), BF16, 1),
            ((8, D), F32),
            ((channels, LANES), F32),
        ],
        [
            Part(
                (count, 2 * total // BLOCK, 2 * LANES),
                lambda refs, buffer: [(refs[0].at[:, pl.ds(own, 2 * total // BLOCK)], buffer)],
            ),
            *([whole] * 4),
            late,
            late,
            "v",
            late,
        ],
        [((total, 2 * LANES), F32), ((3 * LANES, D), BF16)],
    )(mixed_own, gate_pre, grad_y, slope, gate_hat, up_own, hat, ln_mlp_gain, from_attn)
    sibling = moved(apart, "tm", 1)
    pre, joined_all = lax.optimization_barrier((pre, joined_all))
    (late_pack,) = kernel_call(
        late_pack_kernel,
        [((quarters, late_rows, LANES), BF16, 1)],
        [
            Part(
                (total, 2 * LANES),
                lambda refs, buffer: [(refs[0].at[:, pl.ds(LANES, 2 * LANES)], buffer)],
            ),
            whole,
            whole,
            whole,
            blocks_part(1),
            *"vvvvv",
        ],
    )(pre, n_mlp, joined_all, branch, *blocks, vectors, up_columns, first_lines, head_lines, own_lines)
    late_pack, head_parts = lax.optimization_barrier((late_pack, head_parts))
    late_moved = lax.all_to_all(late_pack, "stream", 0, 0, tiled=True)
    (early_part,) = kernel_call(add_kernel, [((4 * HEAD + 8 * share, LANES), BF16)], quarters * "v", megas=24)(
        *head_parts
    )
    early_near = near_blocks(early_part)
    pairs = kernel_call(pair_kernel, [((own, D), BF16)] * (count // 2), "vv", megas=24)(same, sibling)
    sums = [pairs[0]] + [moved(pairs[slot], "tm", 2 * slot) for slot in range(1, count // 2)]
    late_moved, early_near, sums[1], sums[2] = lax.optimization_barrier((late_moved, early_near, sums[1], sums[2]))
    (late_part,) = kernel_call(add_streams_kernel, [((late_rows, LANES), BF16)], "v", megas=24)(late_moved)
    late_near = near_blocks(late_part)
    early_all = far_stack(early_near)
    grad_qkv, grad_pos, grad_down, half_up = kernel_call(
        early_kernel,
        [
            ((quarter, 3 * D), F32),
            ((quarter, D), F32),
            ((HALF // quarters, D), F32),
            ((quarter, 2 * HALF), F32, 1, (quarter, HALF), lambda ref: ref.at[:, pl.ds(0, HALF)]),
        ],
        "vv",
        [((count, 4 * HEAD + 8 * share, LANES), BF16)],
        megas=24,
    )(*early_all)
    late_near, grad_pos, sums = lax.optimization_barrier((late_near, grad_pos, sums))
    late_parts = far_stack(late_near)
    (grad_frames,) = kernel_call(frames_kernel, [((own, D), F32)], (2 + count // 2) * "v", megas=24)(
        own_frames, own_cotangent, *sums
    )
    late_parts, grad_frames = lax.optimization_barrier((late_parts, grad_frames))
    late = kernel_call(
        late_kernel,
        [((quarter,), F32)] * 6
        + [
            ((quarter, D), F32),
            ((quarter, 2 * HALF), F32, 1, (quarter, HALF), lambda ref: ref.at[:, pl.ds(HALF, HALF)]),
            ((2 * HALF // quarters,), F32),
            ((HALF // quarters,), F32),
            ((HALF // quarters,), F32),
            ((KERNEL, HALF // quarters), F32),
            ((HALF // quarters,), F32),
            ((quarter,), F32),
            ((2 * D // quarters, D), F32),
            ((quarter,), F32),
        ],
        "kvv",
        [((count,) + late_part.shape, BF16)],
        megas=24,
        aliases={0: 7},
    )(half_up, *late_parts)
    return (
        out_rows[None],
        grad_frames[None],
        *late[:4],
        grad_qkv,
        *late[4:6],
        grad_pos,
        *late[6:13],
        grad_down,
        *late[13:],
    )


def per_device(*operands):
    fits = (
        lax.axis_size("tm") == HEADS
        and lax.axis_size("stream") * LANES == D
        and operands[0].shape[1] == BLOCK
    )
    return head_device(*operands) if fits else frame_device(*operands)


def solution(mesh):
    return jax.shard_map(
        per_device,
        mesh=mesh,
        in_specs=(
            P("stream", "tm", None),
            P("stream", None),
            P("stream", "tm", None),
            P(),
            P(),
            P(),
            P(),
            P(),
            P(),
            P(),
            P(),
            P(),
            P(),
            P(),
            P(),
            P(),
            P(),
            P(),
            P(),
            P(),
            P(),
            P(),
        ),
        out_specs=(
            P("stream", "tm", None),
            P("stream", "tm", None),
            P("stream"),
            P("stream"),
            P("stream"),
            P("stream"),
            P("stream", None),
            P("stream"),
            P("stream"),
            P("stream", None),
            P("stream", None),
            P("stream", None),
            P("stream"),
            P("stream"),
            P("stream"),
            P(None, "stream"),
            P("stream"),
            P("stream", None),
            P("stream"),
            P("stream", None),
            P("stream"),
        ),
        check_vma=False,
    )
```

```python
import math

import jax
import jax.numpy as jnp
from jax import lax
from jax.experimental import pallas as pl
from jax.experimental.pallas import tpu as pltpu
from jax.sharding import PartitionSpec as P

D = 512
HEADS = 8
HEAD = 64
KERNEL = 31
ITEMS = 5
HALF = 1536


EPS = 1e-05
MASKED = -1e30


def extended(block, sides, width):
    for axis, dim in sides:
        count = lax.axis_size(axis)
        forward = [(i, i + 1) for i in range(count - 1)]
        backward = [(target, source) for source, target in forward]
        low = lax.ppermute(
            lax.slice_in_dim(block, block.shape[dim] - width, None, axis=dim), axis, forward
        )
        high = lax.ppermute(lax.slice_in_dim(block, 0, width, axis=dim), axis, backward)
        block = jnp.concatenate([low, block, high], axis=dim)
    return block


def norm_rows(inputs, scale_row, shift_row):
    row_mean = jnp.mean(inputs, axis=-1, keepdims=True)
    centred = inputs - row_mean
    spread = jnp.mean(centred * centred, axis=-1, keepdims=True)
    return centred * lax.rsqrt(spread + EPS) * scale_row + shift_row


def gelu_exact(inputs):
    return jax.nn.gelu(inputs, approximate=False)


def frame_info(lengths, offset, extent):
    item_ends = jnp.cumsum(lengths)
    first_table = jnp.concatenate([item_ends - lengths, item_ends[-1:]])
    frame_index = offset + jnp.arange(extent, dtype=jnp.int32)
    item_of = jnp.sum((frame_index[:, None] >= item_ends[None, :]).astype(jnp.int32), axis=1)
    labels = jnp.arange(ITEMS + 1, dtype=jnp.int32)
    first_frame = jnp.sum(
        jnp.where(item_of[:, None] == labels[None, :], first_table[None, :], 0), axis=1
    )
    return (frame_index, item_of, frame_index - first_frame)


def angles(place_in):
    frequency = jnp.exp(jnp.arange(D // 2, dtype=jnp.float32) * (-2.0 * math.log(10000.0) / D))
    phase_angle = place_in.astype(jnp.float32)[:, None] * frequency[None, :]
    return (jnp.sin(phase_angle), jnp.cos(phase_angle))


def rel_query(projected, sine_rows, cosine_rows):
    half_size = projected.shape[-1] // 2
    first_half = projected[..., :half_size]
    second_half = projected[..., half_size:]
    sine_wide = sine_rows[:, None, :]
    cosine_wide = cosine_rows[:, None, :]
    return jnp.concatenate(
        [
            first_half * sine_wide + second_half * cosine_wide,
            second_half * sine_wide - first_half * cosine_wide,
        ],
        axis=-1,
    )


def step_size(extent):
    return math.gcd(extent, 512)


def score_block(q_content, q_rel, query_item, query_frame, key_block, key_start, lengths):
    extent = key_block.shape[0]
    key_frame, key_item, key_place = frame_info(lengths, key_start, extent)
    sine_rows, cosine_rows = angles(key_place)
    k_rel = jnp.concatenate([cosine_rows, sine_rows], axis=1).astype(jnp.bfloat16)
    raw_scores = jnp.einsum(
        "qhe,khe->hqk",
        q_content,
        key_block.reshape(extent, HEADS, HEAD),
        preferred_element_type=jnp.float32,
    )
    raw_scores = raw_scores + jnp.einsum(
        "qhc,kc->hqk", q_rel, k_rel, preferred_element_type=jnp.float32
    )
    allowed = (query_item[:, None] == key_item[None, :]) & (
        (query_item[:, None] < ITEMS) | (query_frame[:, None] == key_frame[None, :])
    )
    return (raw_scores, allowed, k_rel)


def block_grads(
    q_content,
    q_rel,
    query_item,
    query_frame,
    grad_out,
    log_total,
    delta_rows,
    key_block,
    value_block,
    key_start,
    lengths,
):
    extent = key_block.shape[0]
    raw_scores, allowed, k_rel = score_block(
        q_content, q_rel, query_item, query_frame, key_block, key_start, lengths
    )
    prob_rows = jnp.where(allowed[None], jnp.exp(raw_scores * 0.125 - log_total[:, :, None]), 0.0)
    grad_prob = jnp.einsum(
        "qhe,khe->hqk",
        grad_out,
        value_block.reshape(extent, HEADS, HEAD),
        preferred_element_type=jnp.float32,
    )
    grad_raw = (prob_rows * (grad_prob - delta_rows[:, :, None]) * 0.125).astype(jnp.bfloat16)
    return (prob_rows.astype(jnp.bfloat16), grad_raw, k_rel)


def frame_device(
    frames,
    lengths,
    cotangent,
    ln_attn_gain,
    ln_attn_bias,
    ln_mlp_gain,
    ln_mlp_bias,
    qkv_weight,
    content_bias,
    position_bias,
    pos_weight,
    out_weight,
    up_weight,
    up_bias,
    gate_norm_gain,
    gate_norm_bias,
    conv_kernel,
    conv_bias,
    down_weight,
    down_bias,
    merge_weight,
    merge_bias,
):
    row_count = frames.shape[1]
    cycle_size = lax.axis_size("tm")
    offset = lax.axis_index("tm") * row_count
    stream_lengths = lengths[0]
    inputs = frames[0].astype(jnp.float32)
    frame_index, item_of, place_in = frame_info(stream_lengths, offset, row_count)
    sine_rows, cosine_rows = angles(place_in)
    attn_norm, attn_pull = jax.vjp(
        norm_rows, inputs, ln_attn_gain.astype(jnp.float32), ln_attn_bias.astype(jnp.float32)
    )
    mlp_norm, mlp_pull = jax.vjp(
        norm_rows, inputs, ln_mlp_gain.astype(jnp.float32), ln_mlp_bias.astype(jnp.float32)
    )
    attn_norm_low = attn_norm.astype(jnp.bfloat16)
    mlp_norm_low = mlp_norm.astype(jnp.bfloat16)
    qkv_rows = jnp.dot(attn_norm_low, qkv_weight, preferred_element_type=jnp.float32)
    query_rows = qkv_rows[:, :D]
    key_rows = qkv_rows[:, D : 2 * D].astype(jnp.bfloat16)
    value_rows = qkv_rows[:, 2 * D :].astype(jnp.bfloat16)
    q_content = (query_rows + content_bias.astype(jnp.float32)).astype(jnp.bfloat16)
    q_position = (query_rows + position_bias.astype(jnp.float32)).astype(jnp.bfloat16)
    content_heads = q_content.reshape(row_count, HEADS, HEAD)
    position_heads = q_position.reshape(row_count, HEADS, HEAD)
    pos_heads = pos_weight.reshape(D, HEADS, HEAD)
    projected = jnp.einsum(
        "the,che->thc", position_heads, pos_heads, preferred_element_type=jnp.float32
    )
    q_rel = rel_query(projected, sine_rows, cosine_rows).astype(jnp.bfloat16)
    start_state = (
        jnp.full((HEADS, row_count), MASKED, jnp.float32),
        jnp.zeros((HEADS, row_count), jnp.float32),
        jnp.zeros((HEADS, row_count, HEAD), jnp.float32),
    )
    fold_state = start_state
    key_piece = lax.all_gather(key_rows, "tm", axis=0, tiled=True)
    value_piece = lax.all_gather(value_rows, "tm", axis=0, tiled=True)
    extent = key_piece.shape[0]
    step_rows = step_size(extent)

    def forward_one_step(inner_state, step_index):
        row_top, row_total, row_acc = inner_state
        key_block = lax.dynamic_slice_in_dim(key_piece, step_index * step_rows, step_rows, 0)
        value_block = lax.dynamic_slice_in_dim(value_piece, step_index * step_rows, step_rows, 0)
        raw_scores, allowed, k_rel = score_block(
            content_heads,
            q_rel,
            item_of,
            frame_index,
            key_block,
            step_index * step_rows,
            stream_lengths,
        )
        scaled = jnp.where(allowed[None], raw_scores * 0.125, MASKED)
        new_top = jnp.maximum(row_top, jnp.max(scaled, axis=2))
        weight = jnp.where(allowed[None], jnp.exp(scaled - new_top[:, :, None]), 0.0)
        factor = jnp.exp(row_top - new_top)
        row_total = row_total * factor + jnp.sum(weight, axis=2)
        row_acc = row_acc * factor[:, :, None] + jnp.einsum(
            "hqk,khe->hqe",
            weight.astype(jnp.bfloat16),
            value_block.reshape(step_rows, HEADS, HEAD),
            preferred_element_type=jnp.float32,
        )
        return ((new_top, row_total, row_acc), None)

    fold_state, unused = lax.scan(
        forward_one_step, fold_state, jnp.arange(extent // step_rows, dtype=jnp.int32)
    )
    row_top, row_total, row_acc = fold_state
    attn_heads = row_acc / row_total[:, :, None]
    log_total = row_top + jnp.log(row_total)
    attn_low = jnp.transpose(attn_heads, (1, 0, 2)).reshape(row_count, D).astype(jnp.bfloat16)
    branch_attn = jnp.dot(attn_low, out_weight, preferred_element_type=jnp.float32).astype(
        jnp.bfloat16
    )
    hidden_pre = jnp.dot(
        mlp_norm_low, up_weight, preferred_element_type=jnp.float32
    ) + up_bias.astype(jnp.float32)
    hidden, gelu_pull = jax.vjp(gelu_exact, hidden_pre)
    gate_half = hidden[:, :HALF]
    conv_norm, conv_pull = jax.vjp(
        norm_rows,
        hidden[:, HALF:],
        gate_norm_gain.astype(jnp.float32),
        gate_norm_bias.astype(jnp.float32),
    )
    conv_in = conv_norm.astype(jnp.bfloat16)
    half_width = KERNEL // 2
    conv_wide = extended(conv_in, (("tm", 0),), half_width)
    wide_frame, wide_item, wide_place = frame_info(
        stream_lengths, offset - half_width, row_count + 2 * half_width
    )
    kernel_rows = conv_kernel.astype(jnp.float32)
    conv_out = conv_bias.astype(jnp.float32) + jnp.zeros_like(gate_half)
    for tap_index in range(KERNEL):
        same_item = (wide_item[tap_index : tap_index + row_count] == item_of)[:, None]
        conv_out = (
            conv_out
            + jnp.where(
                same_item, conv_wide[tap_index : tap_index + row_count].astype(jnp.float32), 0.0
            )
            * kernel_rows[tap_index]
        )
    gated_low = (gate_half * conv_out).astype(jnp.bfloat16)
    branch_mlp = (
        jnp.dot(gated_low, down_weight, preferred_element_type=jnp.float32)
        + down_bias.astype(jnp.float32)
    ).astype(jnp.bfloat16)
    joined = jnp.concatenate([branch_attn, branch_mlp], axis=1)
    result = (
        inputs
        + jnp.dot(joined, merge_weight, preferred_element_type=jnp.float32)
        + merge_bias.astype(jnp.float32)
    )
    out_rows = result.astype(jnp.bfloat16)[None]
    grad_low = cotangent[0]
    grad_rows = grad_low.astype(jnp.float32)
    grad_merge_bias = jnp.sum(grad_rows, axis=0)
    grad_merge_weight = jnp.einsum(
        "tc,td->cd", joined, grad_low, preferred_element_type=jnp.float32
    )
    grad_joined = jnp.einsum(
        "td,cd->tc", grad_low, merge_weight, preferred_element_type=jnp.float32
    )
    grad_attn_branch = grad_joined[:, :D].astype(jnp.bfloat16)
    grad_mlp_branch = grad_joined[:, D:].astype(jnp.bfloat16)
    grad_down_weight = jnp.einsum(
        "tc,td->cd", gated_low, grad_mlp_branch, preferred_element_type=jnp.float32
    )
    grad_down_bias = jnp.sum(grad_mlp_branch.astype(jnp.float32), axis=0)
    grad_gated = jnp.einsum(
        "td,cd->tc", grad_mlp_branch, down_weight, preferred_element_type=jnp.float32
    )
    grad_gate_half = grad_gated * conv_out
    grad_conv_out = (grad_gated * gate_half).astype(jnp.bfloat16)
    grad_conv_rows = grad_conv_out.astype(jnp.float32)
    grad_conv_bias = jnp.sum(grad_conv_rows, axis=0)
    grad_wide = extended(grad_conv_out, (("tm", 0),), half_width)
    kernel_list = []
    grad_conv_in = jnp.zeros_like(grad_conv_rows)
    for tap_index in range(KERNEL):
        same_item = (wide_item[tap_index : tap_index + row_count] == item_of)[:, None]
        kernel_list.append(
            jnp.sum(
                jnp.where(
                    same_item, conv_wide[tap_index : tap_index + row_count].astype(jnp.float32), 0.0
                )
                * grad_conv_rows,
                axis=0,
            )
        )
        back_start = 2 * half_width - tap_index
        back_item = (wide_item[back_start : back_start + row_count] == item_of)[:, None]
        grad_conv_in = (
            grad_conv_in
            + jnp.where(
                back_item, grad_wide[back_start : back_start + row_count].astype(jnp.float32), 0.0
            )
            * kernel_rows[tap_index]
        )
    grad_conv_kernel = jnp.stack(kernel_list)
    grad_second, grad_gate_norm_gain, grad_gate_norm_bias = conv_pull(grad_conv_in)
    (grad_pre_rows,) = gelu_pull(jnp.concatenate([grad_gate_half, grad_second], axis=1))
    grad_pre = grad_pre_rows.astype(jnp.bfloat16)
    grad_up_bias = jnp.sum(grad_pre.astype(jnp.float32), axis=0)
    grad_up_weight = jnp.einsum(
        "tc,tf->cf", mlp_norm_low, grad_pre, preferred_element_type=jnp.float32
    )
    grad_mlp_norm = jnp.einsum("tf,cf->tc", grad_pre, up_weight, preferred_element_type=jnp.float32)
    grad_out_weight = jnp.einsum(
        "tc,td->cd", attn_low, grad_attn_branch, preferred_element_type=jnp.float32
    )
    grad_attn_low = jnp.einsum(
        "td,cd->tc", grad_attn_branch, out_weight, preferred_element_type=jnp.float32
    ).astype(jnp.bfloat16)
    grad_out_heads = grad_attn_low.reshape(row_count, HEADS, HEAD)
    delta_rows = jnp.sum(
        jnp.transpose(grad_out_heads.astype(jnp.float32), (1, 0, 2)) * attn_heads, axis=2
    )
    total_frames = row_count * cycle_size
    back_start_state = (
        jnp.zeros((row_count, HEADS, HEAD), jnp.float32),
        jnp.zeros((row_count, HEADS, D), jnp.float32),
        jnp.zeros((total_frames, D), jnp.float32),
        jnp.zeros((total_frames, D), jnp.float32),
    )
    back_key_piece = lax.all_gather(key_rows, "tm", axis=0, tiled=True)
    back_value_piece = lax.all_gather(value_rows, "tm", axis=0, tiled=True)
    extent = back_key_piece.shape[0]
    back_step_rows = step_size(extent)

    def back_one_step(inner_state, step_index):
        grad_content, grad_rel = inner_state
        key_block = lax.dynamic_slice_in_dim(
            back_key_piece, step_index * back_step_rows, back_step_rows, 0
        )
        value_block = lax.dynamic_slice_in_dim(
            back_value_piece, step_index * back_step_rows, back_step_rows, 0
        )
        prob_low, grad_raw, k_rel = block_grads(
            content_heads,
            q_rel,
            item_of,
            frame_index,
            grad_out_heads,
            log_total,
            delta_rows,
            key_block,
            value_block,
            step_index * back_step_rows,
            stream_lengths,
        )
        grad_content = grad_content + jnp.einsum(
            "hqk,khe->qhe",
            grad_raw,
            key_block.reshape(back_step_rows, HEADS, HEAD),
            preferred_element_type=jnp.float32,
        )
        grad_rel = grad_rel + jnp.einsum(
            "hqk,kc->qhc", grad_raw, k_rel, preferred_element_type=jnp.float32
        )
        key_part = jnp.einsum(
            "hqk,qhe->khe", grad_raw, content_heads, preferred_element_type=jnp.float32
        ).reshape(back_step_rows, D)
        value_part = jnp.einsum(
            "hqk,qhe->khe", prob_low, grad_out_heads, preferred_element_type=jnp.float32
        ).reshape(back_step_rows, D)
        return ((grad_content, grad_rel), (key_part, value_part))

    inner_state, block_parts = lax.scan(
        back_one_step,
        (back_start_state[0], back_start_state[1]),
        jnp.arange(extent // back_step_rows, dtype=jnp.int32),
    )
    key_all = block_parts[0].reshape(extent, D)
    value_all = block_parts[1].reshape(extent, D)
    grad_content, grad_rel, key_all, value_all = (
        inner_state[0],
        inner_state[1],
        key_all,
        value_all,
    )
    grad_keys, grad_values = (
        lax.psum_scatter(key_all, "tm", scatter_dimension=0, tiled=True),
        lax.psum_scatter(value_all, "tm", scatter_dimension=0, tiled=True),
    )
    half_size = D // 2
    rel_first = grad_rel[..., :half_size]
    rel_second = grad_rel[..., half_size:]
    sine_wide = sine_rows[:, None, :]
    cosine_wide = cosine_rows[:, None, :]
    grad_projected = jnp.concatenate(
        [
            rel_first * sine_wide - rel_second * cosine_wide,
            rel_first * cosine_wide + rel_second * sine_wide,
        ],
        axis=-1,
    ).astype(jnp.bfloat16)
    grad_pos_weight = jnp.einsum(
        "thc,the->che", grad_projected, position_heads, preferred_element_type=jnp.float32
    ).reshape(D, D)
    grad_q_position = jnp.einsum(
        "thc,che->the", grad_projected, pos_heads, preferred_element_type=jnp.float32
    )
    grad_content_bias = jnp.sum(grad_content, axis=0).reshape(D)
    grad_position_bias = jnp.sum(grad_q_position, axis=0).reshape(D)
    grad_query = (grad_content + grad_q_position).reshape(row_count, D).astype(jnp.bfloat16)
    grad_qkv = jnp.concatenate(
        [grad_query, grad_keys.astype(jnp.bfloat16), grad_values.astype(jnp.bfloat16)], axis=1
    )
    grad_qkv_weight = jnp.einsum(
        "tc,tf->cf", attn_norm_low, grad_qkv, preferred_element_type=jnp.float32
    )
    grad_attn_norm = jnp.einsum(
        "tf,cf->tc", grad_qkv, qkv_weight, preferred_element_type=jnp.float32
    )
    grad_from_attn, grad_ln_attn_gain, grad_ln_attn_bias = attn_pull(grad_attn_norm)
    grad_from_mlp, grad_ln_mlp_gain, grad_ln_mlp_bias = mlp_pull(grad_mlp_norm)
    grad_inputs = grad_rows + grad_from_attn + grad_from_mlp
    weight_grads = (
        grad_ln_attn_gain,
        grad_ln_attn_bias,
        grad_ln_mlp_gain,
        grad_ln_mlp_bias,
        grad_qkv_weight,
        grad_content_bias,
        grad_position_bias,
        grad_pos_weight,
        grad_out_weight,
        grad_up_weight,
        grad_up_bias,
        grad_gate_norm_gain,
        grad_gate_norm_bias,
        grad_conv_kernel,
        grad_conv_bias,
        grad_down_weight,
        grad_down_bias,
        grad_merge_weight,
        grad_merge_bias,
    )
    summed = lax.psum(
        (
            weight_grads[0],
            weight_grads[1],
            weight_grads[2],
            weight_grads[3],
            weight_grads[4],
            weight_grads[5],
            weight_grads[6],
            weight_grads[7],
            weight_grads[8],
            weight_grads[9],
            weight_grads[10],
            weight_grads[11],
            weight_grads[12],
            weight_grads[13],
            weight_grads[14],
            weight_grads[15],
            weight_grads[16],
            weight_grads[17],
            weight_grads[18],
        ),
        "tm",
    )
    shares = (
        lax.psum_scatter(
            summed[0].astype(jnp.bfloat16), "stream", scatter_dimension=0, tiled=True
        ).astype(jnp.float32),
        lax.psum_scatter(
            summed[1].astype(jnp.bfloat16), "stream", scatter_dimension=0, tiled=True
        ).astype(jnp.float32),
        lax.psum_scatter(
            summed[2].astype(jnp.bfloat16), "stream", scatter_dimension=0, tiled=True
        ).astype(jnp.float32),
        lax.psum_scatter(
            summed[3].astype(jnp.bfloat16), "stream", scatter_dimension=0, tiled=True
        ).astype(jnp.float32),
        lax.psum_scatter(
            summed[4].astype(jnp.bfloat16), "stream", scatter_dimension=0, tiled=True
        ).astype(jnp.float32),
        lax.psum_scatter(
            summed[5].astype(jnp.bfloat16), "stream", scatter_dimension=0, tiled=True
        ).astype(jnp.float32),
        lax.psum_scatter(
            summed[6].astype(jnp.bfloat16), "stream", scatter_dimension=0, tiled=True
        ).astype(jnp.float32),
        lax.psum_scatter(
            summed[7].astype(jnp.bfloat16), "stream", scatter_dimension=0, tiled=True
        ).astype(jnp.float32),
        lax.psum_scatter(
            summed[8].astype(jnp.bfloat16), "stream", scatter_dimension=0, tiled=True
        ).astype(jnp.float32),
        lax.psum_scatter(
            summed[9].astype(jnp.bfloat16), "stream", scatter_dimension=0, tiled=True
        ).astype(jnp.float32),
        lax.psum_scatter(
            summed[10].astype(jnp.bfloat16), "stream", scatter_dimension=0, tiled=True
        ).astype(jnp.float32),
        lax.psum_scatter(
            summed[11].astype(jnp.bfloat16), "stream", scatter_dimension=0, tiled=True
        ).astype(jnp.float32),
        lax.psum_scatter(
            summed[12].astype(jnp.bfloat16), "stream", scatter_dimension=0, tiled=True
        ).astype(jnp.float32),
        lax.psum_scatter(
            summed[13].astype(jnp.bfloat16), "stream", scatter_dimension=1, tiled=True
        ).astype(jnp.float32),
        lax.psum_scatter(
            summed[14].astype(jnp.bfloat16), "stream", scatter_dimension=0, tiled=True
        ).astype(jnp.float32),
        lax.psum_scatter(
            summed[15].astype(jnp.bfloat16), "stream", scatter_dimension=0, tiled=True
        ).astype(jnp.float32),
        lax.psum_scatter(
            summed[16].astype(jnp.bfloat16), "stream", scatter_dimension=0, tiled=True
        ).astype(jnp.float32),
        lax.psum_scatter(
            summed[17].astype(jnp.bfloat16), "stream", scatter_dimension=0, tiled=True
        ).astype(jnp.float32),
        lax.psum_scatter(
            summed[18].astype(jnp.bfloat16), "stream", scatter_dimension=0, tiled=True
        ).astype(jnp.float32),
    )
    return (out_rows, grad_inputs[None]) + tuple(shares)


LANES = 128
LOW = LANES // 2
BLOCK = 128
TALL = 256
WINDOW = 64
MARGIN = 16
BOUNDS = 16
MEGA = 1024 * 1024
F32 = jnp.float32
BF16 = jnp.bfloat16


def dot_nn(left, right):
    return jnp.dot(left, right, preferred_element_type=F32)


def dot_nt(left, right):
    return lax.dot_general(left, right, (((1,), (1,)), ((), ())), preferred_element_type=F32)


def dot_tn(left, right):
    return lax.dot_general(left, right, (((0,), (0,)), ((), ())), preferred_element_type=F32)


def rows_of(index, size, base=0):
    return pl.ds(pl.multiple_of(index * size, size) + base, size)


def line_of(ref):
    return ref[...].astype(F32).reshape(1, ref.shape[0])


def fold_rows(values):
    return jnp.sum(values.reshape(values.shape[0] // 8, 8, values.shape[1]), axis=0)


def one_row(values):
    return jnp.sum(values, axis=0, keepdims=True)


def turn(values):
    return pltpu.roll(values, LOW, 1)


def low_lanes(rows):
    return lax.broadcasted_iota(jnp.int32, (rows, LANES), 1) < LOW


def centre_rows(inputs):
    mean = jnp.mean(inputs, axis=-1, keepdims=True)
    centred = inputs - mean
    spread = jnp.mean(centred * centred, axis=-1, keepdims=True)
    return centred * lax.rsqrt(spread + EPS)


def gelu_parts(values):
    phi = 0.5 + 0.5 * lax.erf(values * math.sqrt(0.5))
    bell = jnp.exp(values * values * -0.5)
    return values * phi, phi + values * bell * (1.0 / math.sqrt(2.0 * math.pi))


class Part:
    def __init__(self, shape=None, pairs=None, refs=1, late=False):
        self.shape, self.pairs, self.refs, self.late = shape, pairs, refs, late

    def buffer(self, operand):
        return self.shape or operand.shape

    def copies(self, refs, buffer):
        return self.pairs(refs, buffer) if self.pairs else [(refs[0], buffer)]


def blocks_part(half, late=False):
    def pairs(refs, buffer):
        place = lax.axis_index("tm")
        return [
            (
                ref.at[:, pl.ds(half * D, D)],
                buffer.at[rows_of(lax.bitwise_xor(jnp.int32(apart), place), BLOCK)],
            )
            for apart, ref in enumerate(refs)
        ]

    return Part((HEADS * BLOCK, D), pairs, HEADS, late)


def rows_part(first, size, late=False):
    return Part((size, D), lambda refs, buffer: [(refs[0].at[pl.ds(first, size)], buffer)], late=late)


class Fetch:
    def __init__(self, pairs, buffer, sems, first):
        self.buffer, self.begun = buffer, False
        self.pending = [
            pltpu.make_async_copy(source, target, sems.at[first + index])
            for index, (source, target) in enumerate(pairs)
        ]

    def begin(self):
        if not self.begun:
            for copy in self.pending:
                copy.start()
        self.begun = True

    def __call__(self):
        self.begin()
        for copy in self.pending:
            copy.wait()
        self.pending = []
        return self.buffer


def begin(*fetches):
    for fetch in fetches:
        fetch.begin()


class Send:
    def __init__(self, buffer, target, sems):
        self.buffer, self.target, self.sems, self.copies = buffer, target, sems, []

    def go(self, *index):
        source, target = (self.buffer.at[index], self.target.at[index]) if index else (self.buffer, self.target)
        copy = pltpu.make_async_copy(source, target, self.sems[len(self.copies)])
        copy.start()
        self.copies.append(copy)

    def finish(self):
        if not self.copies:
            self.go()


SPACES = {"v": pltpu.VMEM, "s": pltpu.SMEM, "k": pl.ANY}


def kernel_call(body, out_shapes, plan, scratch=(), megas=58, bounds=False, aliases=None):
    def call(*operands):
        in_specs, buffers, at = [], [], 0
        for item in plan:
            if item == "f":
                in_specs.append(pl.BlockSpec(memory_space=pl.ANY))
                buffers.append(pltpu.VMEM(operands[at].shape, operands[at].dtype))
                at += 1
            elif isinstance(item, Part):
                in_specs += [pl.BlockSpec(memory_space=pl.ANY)] * item.refs
                buffers.append(pltpu.VMEM(item.buffer(operands[at]), operands[at].dtype))
                at += item.refs
            else:
                in_specs.append(pl.BlockSpec(memory_space=SPACES[item]))
                at += 1
        sent = [out for out in out_shapes if len(out) > 2]
        buffers += [pltpu.VMEM(out[3] if len(out) > 3 else out[0], out[1]) for out in sent]
        sem_count = 96
        extra = [pltpu.SMEM((BOUNDS,), jnp.int32)] if bounds else []

        def outer(*refs):
            inputs, rest = refs[: len(in_specs)], refs[len(in_specs) :]
            outputs, rest = rest[: len(out_shapes)], rest[len(out_shapes) :]
            held, rest = list(rest[: len(buffers)]), rest[len(buffers) :]
            sems, rest = rest[0], rest[1:]
            given, at, used = [], 0, 0
            for item in plan:
                if item == "f":
                    given.append(Fetch([(inputs[at], held[0])], held.pop(0), sems, used))
                    given[-1].begin()
                    used += 1
                    at += 1
                elif isinstance(item, Part):
                    buffer = held.pop(0)
                    pairs = item.copies(inputs[at : at + item.refs], buffer)
                    given.append(Fetch(pairs, buffer, sems, used))
                    if not item.late:
                        given[-1].begin()
                    used += len(pairs)
                    at += item.refs
                else:
                    given.append(inputs[at])
                    at += 1
            results = []
            for out, ref in zip(out_shapes, outputs):
                if len(out) > 2:
                    target = out[4](ref) if len(out) > 3 else ref
                    results.append(Send(held.pop(0), target, [sems.at[used + index] for index in range(4)]))
                    used += 4
                else:
                    results.append(ref)
            assert used <= sem_count
            given = [item() if kind == "f" else item for kind, item in zip(plan, given)]
            body(*given, *results, *rest)
            for item in given:
                if isinstance(item, Fetch):
                    item()
            sends = [item for item in results if isinstance(item, Send)]
            for item in sends:
                item.finish()
            for item in sends:
                for copy in item.copies:
                    copy.wait()

        return pl.pallas_call(
            outer,
            out_shape=[jax.ShapeDtypeStruct(out[0], out[1]) for out in out_shapes],
            in_specs=in_specs,
            out_specs=[pl.BlockSpec(memory_space=pl.ANY if len(out) > 2 else pltpu.VMEM) for out in out_shapes],
            scratch_shapes=buffers
            + [pltpu.SemaphoreType.DMA((sem_count,))]
            + [pltpu.VMEM(shape, kind) for shape, kind in scratch]
            + extra,
            input_output_aliases=aliases or {},
            compiler_params=pltpu.CompilerParams(vmem_limit_bytes=megas * MEGA),
            cost_estimate=pl.CostEstimate(flops=0, bytes_accessed=0, transcendentals=0),
        )(*operands)

    return call


def fill_bounds(lengths_ref, bounds_s, total):
    bounds_s[0] = jnp.int32(0)
    end = jnp.int32(0)
    for item in range(ITEMS):
        end = end + lengths_ref[0, item]
        bounds_s[item + 1] = end
    for item in range(ITEMS + 1, BOUNDS):
        bounds_s[item] = jnp.int32(total)


def select_kernel(
    up_ref,
    up_bias_ref,
    gain_ref,
    bias_ref,
    conv_bias_ref,
    taps_ref,
    qkv_ref,
    pos_ref,
    content_ref,
    position_ref,
    up_out,
    table_out,
    qkv_out,
    pos_out,
    bias_out,
):
    place = lax.axis_index("tm")
    quarters = lax.axis_size("stream")
    share = HALF // (quarters * lax.axis_size("tm"))
    lane = lax.broadcasted_iota(jnp.int32, (1, 2 * LANES), 1)
    channel = jnp.where(lane < LANES + LOW, lane, lane - LOW)
    group = jnp.zeros_like(channel)
    for quarter in range(1, quarters):
        group = group + (channel >= quarter * share).astype(jnp.int32)
    source = group * (HALF // quarters) + share * place + channel - group * share
    chosen = (lax.broadcasted_iota(jnp.int32, (HALF, 2 * LANES), 0) == source).astype(F32).astype(BF16)
    gate = dot_nn(up_ref[:, :HALF], chosen)
    conv = dot_nn(up_ref[:, HALF:], chosen)
    up_out[:, :LANES] = gate[:, :LANES].astype(BF16)
    up_out[:, LANES : 2 * LANES] = jnp.where(low_lanes(D), gate[:, LANES:], conv[:, LANES:]).astype(BF16)
    up_out[:, 2 * LANES :] = conv[:, :LANES].astype(BF16)
    up_bias = line_of(up_bias_ref)
    lines = jnp.concatenate(
        [
            up_bias[:, :HALF],
            up_bias[:, HALF:],
            line_of(gain_ref),
            line_of(bias_ref),
            line_of(conv_bias_ref),
            jnp.zeros((3, HALF), F32),
        ],
        axis=0,
    )
    lines = dot_nn(lines.astype(BF16), chosen)
    taps = dot_nn(taps_ref[...], chosen)
    for part in range(2):
        lanes = slice(part * LANES, (part + 1) * LANES)
        table_out[part, :8] = lines[:, lanes]
        table_out[part, 8 : 8 + KERNEL] = taps[:, lanes]
        table_out[part, 8 + KERNEL :] = jnp.zeros((1, LANES), F32)

    odd = lax.rem(place, 2) == 1

    def head_lanes(ref, base):
        at = pl.ds(pl.multiple_of(lax.div(place, 2) * LANES + base, LANES), LANES)
        values = ref[:, at].astype(F32)
        values = jnp.where(odd, turn(values), values)
        return jnp.where(low_lanes(values.shape[0]), values, 0.0)

    for part in range(3):
        qkv_out[:, part * LANES : (part + 1) * LANES] = head_lanes(qkv_ref, part * D).astype(BF16)
    pos_out[...] = head_lanes(pos_ref, 0).astype(BF16)
    bias_out[...] = jnp.zeros((8, LANES), F32)
    for line, ref in enumerate((content_ref, position_ref)):
        values = line_of(ref)
        picked = values[:, :LANES]
        for tile in range(1, D // LANES):
            picked = jnp.where(
                lax.div(place, 2) == tile, values[:, tile * LANES : (tile + 1) * LANES], picked
            )
        picked = jnp.where(odd, turn(picked), picked)
        bias_out[line : line + 1] = jnp.where(low_lanes(1), picked, 0.0)


def angle_rows(coarse_ref, fine_ref, block, rows):
    half = D // 2
    base = coarse_ref[pl.ds(block, 1)]
    base_sine, base_cosine = base[:, :half], base[:, half:]
    sine, cosine = fine_ref[rows, :half], fine_ref[rows, half:]
    return base_sine * cosine + base_cosine * sine, base_cosine * cosine - base_sine * sine


def item_codes(bounds_s, index):
    code = jnp.zeros_like(index)
    for item in range(1, ITEMS + 1):
        code = code + (index >= bounds_s[item]).astype(jnp.int32)
    return jnp.where(code < ITEMS, code, ITEMS + index)


def attend_kernel(
    lengths_ref,
    x_ref,
    attn_gain_ref,
    attn_bias_ref,
    mlp_gain_ref,
    mlp_bias_ref,
    qkv_ref,
    pos_ref,
    bias_ref,
    coarse_ref,
    fine_ref,
    up_ref,
    up_bias_ref,
    n_attn_out,
    n_mlp_out,
    hat_out,
    q_position_out,
    query_out,
    key_out,
    value_out,
    prob_out,
    attn_out,
    mean_out,
    rate_out,
    query_s,
    bounds_s,
):
    frames = n_attn_out.buffer.shape[0]
    half = D // 2
    fill_bounds(lengths_ref, bounds_s, frames)
    attn_gain, attn_bias = line_of(attn_gain_ref), line_of(attn_bias_ref)
    mlp_gain, mlp_bias = line_of(mlp_gain_ref), line_of(mlp_bias_ref)
    content, position = bias_ref[0:1], bias_ref[1:2]
    x_ref = x_ref()
    begin(up_ref)
    lane = lax.broadcasted_iota(jnp.int32, (1, LANES), 1)
    spare = ((lane == HEAD) | (lane == HEAD + 1)).astype(F32)

    @pl.loop(0, frames // TALL, unroll=4)
    def _(block):
        rows = rows_of(block, TALL)
        for part in range(TALL // 32):
            at = pl.ds(pl.multiple_of(block * TALL + part * 32, 32), 32)
            hat = centre_rows(x_ref[at].astype(F32))
            hat_out.buffer[at] = hat.astype(BF16)
            n_attn_out.buffer[at] = (hat * attn_gain + attn_bias).astype(BF16)
            n_mlp_out.buffer[at] = (hat * mlp_gain + mlp_bias).astype(BF16)
        parts = dot_nn(n_attn_out.buffer[rows], qkv_ref[...])
        query = parts[:, :LANES]
        query_content = ((query + content).astype(BF16).astype(F32) * 0.125).astype(BF16)
        query_out.buffer[rows] = query_content
        query_s[rows, :LANES] = query_content
        q_position = (query + position).astype(BF16)
        q_position_out.buffer[rows] = q_position
        key_out.buffer[rows, :LANES] = parts[:, LANES : 2 * LANES].astype(BF16)
        value_out.buffer[rows] = (parts[:, 2 * LANES :] + spare).astype(BF16)
        projected = dot_nt(q_position, pos_ref[...])
        for part in range(TALL // 32):
            at = pl.ds(pl.multiple_of(block * TALL + part * 32, 32), 32)
            inner = part * 32 % BLOCK
            sine, cosine = angle_rows(
                coarse_ref, fine_ref, block * (TALL // BLOCK) + part * 32 // BLOCK, slice(inner, inner + 32)
            )
            first = projected[part * 32 : part * 32 + 32, :half]
            second = projected[part * 32 : part * 32 + 32, half:]
            query_s[at, LANES : LANES + half] = ((first * sine + second * cosine) * 0.125).astype(BF16)
            query_s[at, LANES + half :] = ((second * sine - first * cosine) * 0.125).astype(BF16)
            key_out.buffer[at, LANES : LANES + half] = cosine.astype(BF16)
            key_out.buffer[at, LANES + half :] = sine.astype(BF16)

    for out in (n_attn_out, n_mlp_out, hat_out, q_position_out, query_out, key_out, value_out):
        out.go()
    up_ref = up_ref()
    up_bias = line_of(up_bias_ref)[:, HALF:]
    @pl.loop(0, frames // TALL, unroll=2)
    def _(block):
        values = dot_nn(n_mlp_out.buffer[rows_of(block, TALL)], up_ref[...])
        for part in range(TALL // 16):
            pre = values[part * 16 : part * 16 + 16] + up_bias
            hidden = pre * (0.5 + 0.5 * lax.erf(pre * math.sqrt(0.5)))
            mean = jnp.mean(hidden, axis=-1, keepdims=True)
            centred = hidden - mean
            rate = lax.rsqrt(jnp.mean(centred * centred, axis=-1, keepdims=True) + EPS)
            at = pl.ds(pl.multiple_of(block * TALL + part * 16, 16), 16)
            mean_out.buffer[at] = jnp.broadcast_to(mean, (16, LANES))
            rate_out.buffer[at] = jnp.broadcast_to(rate, (16, LANES))

    mean_out.go()
    rate_out.go()
    key_code = item_codes(bounds_s, lax.broadcasted_iota(jnp.int32, (1, frames), 1))

    low = low_lanes(32)
    for block in range(frames // TALL):
        rows = pl.ds(block * TALL, TALL)
        raw = dot_nt(query_s[rows], key_out.buffer[...])
        for part in range(TALL // 32):
            start = block * TALL + part * 32
            index = start + lax.broadcasted_iota(jnp.int32, (32, 1), 0)
            scaled = jnp.where(
                item_codes(bounds_s, index) == key_code, raw[part * 32 : part * 32 + 32], MASKED
            )
            weight = jnp.exp(scaled - jnp.max(scaled, axis=1, keepdims=True))
            prob_out.buffer[pl.ds(start, 32)] = weight.astype(BF16)
        prob_out.go(rows)
        attn = dot_nn(prob_out.buffer[rows], value_out.buffer[...])
        for part in range(TALL // 32):
            own = attn[part * 32 : part * 32 + 32]
            share = 1.0 / own[:, HEAD : HEAD + 1]
            attn_out.buffer[pl.ds(block * TALL + part * 32, 32)] = jnp.where(low, own * share, share)


def fill_margins(wide_s, frames):
    edge = jnp.zeros((MARGIN, LANES), F32)
    wide_s[:MARGIN] = edge
    wide_s[MARGIN + frames : 2 * MARGIN + frames] = edge
    base = frames + 3 * MARGIN
    after = base + frames // 2
    low = low_lanes(MARGIN)
    wide_s[base - MARGIN : base] = jnp.where(low, 0.0, turn(wide_s[after - MARGIN : after]))
    wide_s[after : after + MARGIN] = jnp.where(low, turn(wide_s[base : base + MARGIN]), 0.0)


def item_span(bounds_s, frame):
    begin, end = bounds_s[0], bounds_s[BOUNDS - 1]
    for item in range(1, ITEMS + 1):
        edge = bounds_s[item]
        begin = jnp.where(frame >= edge, edge, begin)
    for item in range(ITEMS, 0, -1):
        edge = bounds_s[item]
        end = jnp.where(frame < edge, edge, end)
    return begin, end


def is_whole(bounds_s, start):
    begin, end = item_span(bounds_s, start)
    reach = KERNEL // 2
    low = (begin == 0) | (begin <= start - reach)
    high = (end == bounds_s[BOUNDS - 1]) | (end >= start + WINDOW + reach)
    return low & high & (end >= start + WINDOW)


def tap_limits(bounds_s, start):
    frame = start + lax.broadcasted_iota(jnp.int32, (WINDOW, LANES), 0)
    begin, end = item_span(bounds_s, frame)
    return begin - frame, end - frame


def grouped(values):
    return values.reshape(WINDOW // 8, 8, LANES)


def triple_places(step, frames):
    half = frames // 2
    return (
        pl.multiple_of(step * WINDOW, 2 * MARGIN),
        pl.multiple_of(step * WINDOW + half, 2 * MARGIN),
        pl.multiple_of(step * WINDOW + frames + 2 * MARGIN, 2 * MARGIN),
    )


def over_windows(bounds_s, frames, body):
    half = frames // 2

    @pl.loop(0, half // WINDOW)
    def _(step):
        start = step * WINDOW
        whole = is_whole(bounds_s, start) & is_whole(bounds_s, start + half)

        @pl.when(whole)
        def _():
            body(step, None)

        @pl.when(jnp.logical_not(whole))
        def _():
            first, second = tap_limits(bounds_s, start), tap_limits(bounds_s, start + half)
            low = low_lanes(WINDOW)
            rest = [jnp.where(low, one, other) for one, other in zip(first, second)]
            body(step, (first, second, rest))


def tap_mask(tap, limits):
    shift = tap - KERNEL // 2
    return None if limits is None else (limits[0] <= shift) & (limits[1] > shift)


def tap_view(window_ref, tap, mask):
    view = window_ref[tap + 1 : tap + 1 + WINDOW]
    return grouped(view if mask is None else jnp.where(mask, view, 0.0))


def mlp_first_kernel(
    lengths_ref,
    n_ref,
    up_ref,
    table_ref,
    mean_ref,
    rate_ref,
    cot_ref,
    merge_ref,
    down_ref,
    attn_ref,
    mixed_out,
    gate_pre_out,
    grad_out,
    rate_out,
    hat_out,
    early_out,
    vectors_out,
    lines_out,
    hat_s,
    slope_s,
    gate_s,
    hidden_s,
    gate_slope_s,
    conv_s,
    grad_s,
    out_s,
    back_s,
    branch_s,
    mix_s,
    taps_s,
    turn_s,
    tap_sum_s,
    columns_s,
    forward_s,
    backward_s,
    bounds_s,
):
    place = lax.axis_index("tm")
    frames = mix_s.shape[0]
    half = frames // 2
    blocks = frames // BLOCK
    quarters, early_rows, _ = early_out.buffer.shape
    share = early_rows // 8
    channels = quarters * share
    fill_bounds(lengths_ref, bounds_s, frames)
    for part in range(2):
        for tap in range(KERNEL):
            line = jnp.broadcast_to(table_ref[part, 8 + tap : 9 + tap], (8, LANES))
            taps_s[part, tap] = line
            turn_s[part, KERNEL - 1 - tap] = line
    tap_sum_s[...] = jnp.zeros(tap_sum_s.shape, F32)
    main, rest = table_ref[0, :8], table_ref[1, :8]
    mixed_bias = jnp.where(low_lanes(1), rest[0:1], rest[1:2])
    low = low_lanes(64)
    gate_pre_ref = gate_pre_out.buffer
    n_ref = n_ref()
    mean_ref, rate_ref = mean_ref(), rate_ref()
    begin(cot_ref, merge_ref, down_ref, attn_ref)

    def stat_rows(rows):
        return mean_ref[rows], rate_ref[rows]

    def chunk(start, base=0):
        return pl.ds(pl.multiple_of(start, 64) + base, 64)

    def conv_part(hidden, mean, rate, lines, rows, to_rows):
        hat = (hidden - mean) * rate
        hat_s[rows] = hat
        hat_out.buffer[rows] = hat.astype(BF16)
        conv_s[to_rows] = (hat * lines[2:3] + lines[3:4]).astype(BF16).astype(F32)

    @pl.loop(0, half // TALL, unroll=2)
    def _(block):
        pre = [dot_nn(n_ref[rows_of(block, TALL, base)], up_ref[...]) for base in (0, half)]
        for part in range(TALL // 64):
            inner = slice(part * 64, part * 64 + 64)
            start = block * TALL + part * 64
            mixed = []
            for values, base in zip(pre, (0, half)):
                rows = chunk(start, base)
                gate, gate_slope = gelu_parts(values[inner, :LANES] + main[0:1])
                hidden_s[rows] = gate
                gate_slope_s[rows] = gate_slope
                hidden, slope = gelu_parts(values[inner, 2 * LANES :] + main[1:2])
                mean, rate = stat_rows(rows)
                slope_s[rows] = slope * rate
                conv_part(hidden, mean, rate, main, rows, chunk(start, base + MARGIN))
                mixed.append((*gelu_parts(values[inner, LANES : 2 * LANES] + mixed_bias), mean, rate))
            (low_hidden, low_slope, low_mean, low_rate), (high_hidden, high_slope, high_mean, high_rate) = mixed
            rows = chunk(start, frames)
            hidden_s[rows] = jnp.where(low, low_hidden, turn(high_hidden))
            gate_slope_s[rows] = jnp.where(low, low_slope, turn(high_slope))
            rate = jnp.where(low, low_rate, high_rate)
            slope_s[rows] = jnp.where(low, turn(low_slope), high_slope) * rate
            conv_part(
                jnp.where(low, turn(low_hidden), high_hidden),
                jnp.where(low, low_mean, high_mean),
                rate,
                rest,
                rows,
                chunk(start, frames + 3 * MARGIN),
            )

    hat_out.go()
    fill_margins(conv_s, frames)
    tall = WINDOW + 2 * MARGIN
    outs = (0, half, frames)

    def convolve(step, limits):
        for index, base in enumerate(triple_places(step, frames)):
            forward_s[index] = conv_s[pl.ds(base, tall)]
        for index in range(3):
            own = None if limits is None else limits[index]
            total = jnp.zeros((WINDOW // 8, 8, LANES), F32)
            for tap in range(KERNEL):
                mask = tap_mask(tap, own)
                total = total + tap_view(forward_s.at[index], tap, mask) * taps_s[index // 2, tap][None]
            lines = rest if index == 2 else main
            out_s[rows_of(step, WINDOW, outs[index])] = total.reshape(WINDOW, LANES) + lines[4:5]

    over_windows(bounds_s, frames, convolve)
    cot_ref = cot_ref()
    merge_ref = merge_ref()
    down_ref = down_ref()
    attn_ref = attn_ref()
    down_ref[channels:] = jnp.zeros((2 * LANES - channels, D), BF16)
    zero = jnp.zeros((8, LANES), F32)

    def branch_part(grad_gated, rows, to_rows, sums):
        up_sum, conv_sum = sums
        gate, conv = hidden_s[rows], out_s[rows]
        gate_pre = (grad_gated * conv * gate_slope_s[rows]).astype(BF16)
        gate_pre_ref[rows] = gate_pre
        grad_conv = (grad_gated * gate).astype(BF16).astype(F32)
        grad_s[to_rows] = grad_conv
        gate_pre = gate_pre.astype(F32)
        return gate * conv, gate_pre, (up_sum + fold_rows(gate_pre), conv_sum + fold_rows(grad_conv))

    def branch_step(block, sums):
        main_sums, rest_sums = sums
        grads = []
        for base in (0, half):
            rows = rows_of(block, TALL, base)
            branch = dot_nt(cot_ref[rows], merge_ref[...]).astype(BF16)
            branch_s[rows] = branch
            grads.append(dot_nt(branch, down_ref[...]))
        for part in range(TALL // 64):
            inner = slice(part * 64, part * 64 + 64)
            start = block * TALL + part * 64
            for values, base in zip(grads, (0, half)):
                rows = chunk(start, base)
                gated, gate_pre, main_sums = branch_part(
                    values[inner, :LANES], rows, chunk(start, base + MARGIN), main_sums
                )
                mix_s[rows, :LANES] = gated.astype(BF16)
                gate_s[rows, :LANES] = gate_pre.astype(BF16)
            grad = jnp.where(low, grads[0][inner, LANES:], turn(grads[1][inner, LANES:]))
            gated, gate_pre, rest_sums = branch_part(
                grad, chunk(start, frames), chunk(start, frames + 3 * MARGIN), rest_sums
            )
            low_rows, high_rows = chunk(start), chunk(start, half)
            gate_s[low_rows, LANES:] = gate_pre.astype(BF16)
            gate_s[high_rows, LANES:] = turn(gate_pre).astype(BF16)
            mix_s[low_rows, LANES:] = jnp.where(low, gated, turn(attn_ref[low_rows])).astype(BF16)
            mix_s[high_rows, LANES:] = jnp.where(low, turn(gated), turn(attn_ref[high_rows])).astype(BF16)
        return main_sums, rest_sums

    (main_up, main_conv), (rest_up, rest_conv) = lax.fori_loop(
        0, half // TALL, branch_step, ((zero, zero), (zero, zero)), unroll=2
    )
    gate_pre_out.go()
    fill_margins(grad_s, frames)
    own = rows_of(place, BLOCK)
    lines_out[0:1] = one_row(fold_rows(branch_s[own].astype(F32)))
    lines_out[1:2] = one_row(fold_rows(cot_ref[own].astype(F32)))
    lines_out[2:8] = jnp.zeros((6, D), F32)
    grad_down = dot_tn(mix_s[...], branch_s[...])
    grad_gate = dot_tn(gate_s[...], n_ref[...])
    for quarter in range(quarters):
        for tile in range(4):
            early_out.buffer[quarter, tile * share : (tile + 1) * share] = grad_down[
                quarter * share : (quarter + 1) * share, tile * LANES : (tile + 1) * LANES
            ].astype(BF16)
        early_out.buffer[quarter, 4 * share :] = grad_gate[
            :channels, quarter * LANES : (quarter + 1) * LANES
        ].astype(BF16)
    early_out.go()
    for block in range(blocks):
        mixed_out.buffer[block, :BLOCK] = mix_s[block * BLOCK : (block + 1) * BLOCK]
    mixed_out.go(slice(None), pl.ds(0, BLOCK))

    def differentiate(step, limits):
        for index, base in enumerate(triple_places(step, frames)):
            forward_s[index] = conv_s[pl.ds(base, tall)]
            backward_s[index] = grad_s[pl.ds(base, tall)]
        for index in range(3):
            own = None if limits is None else limits[index]
            total = jnp.zeros((WINDOW // 8, 8, LANES), F32)
            centre = grouped(backward_s[index, MARGIN : MARGIN + WINDOW])
            for tap in range(KERNEL):
                mask = tap_mask(tap, own)
                total = total + tap_view(backward_s.at[index], tap, mask) * turn_s[index // 2, tap][None]
                tap_sum_s[index // 2, tap] += jnp.sum(tap_view(forward_s.at[index], tap, mask) * centre, axis=0)
            back_s[rows_of(step, WINDOW, outs[index])] = total.reshape(WINDOW, LANES)

    over_windows(bounds_s, frames, differentiate)
    lane = lax.broadcasted_iota(jnp.int32, (64, LANES), 1)

    def norm_part(rows, lines, sums):
        gain_sum, bias_sum = sums
        back, hat, slope = back_s[rows], hat_s[rows], slope_s[rows]
        grad = back * lines[2:3]
        grad_out.buffer[rows] = (grad * slope).astype(BF16)
        rate_out.buffer[rows] = slope.astype(BF16)
        along = back * hat
        return grad, along * lines[2:3], (gain_sum + fold_rows(along), bias_sum + fold_rows(back))

    def norm_step(block, sums):
        main_sums, rest_sums = sums
        for part in range(TALL // 64):
            start = block * TALL + part * 64
            pairs = []
            for base in (0, half):
                plain, along, main_sums = norm_part(chunk(start, base), main, main_sums)
                pairs.append([plain, along])
            plain, along, rest_sums = norm_part(chunk(start, frames), rest, rest_sums)
            for item, values in enumerate((plain, along)):
                pairs[0][item] = pairs[0][item] + jnp.where(low, values, 0.0)
                pairs[1][item] = pairs[1][item] + jnp.where(low, 0.0, values)
            for (plain, along), base in zip(pairs, (0, half)):
                columns_s[chunk(start, base)] = jnp.where(
                    lane == 0,
                    jnp.sum(plain, axis=-1, keepdims=True),
                    jnp.where(lane == 1, jnp.sum(along, axis=-1, keepdims=True), 0.0),
                )
        return main_sums, rest_sums

    (main_gain, main_bias), (rest_gain, rest_bias) = lax.fori_loop(
        0, half // TALL, norm_step, ((zero, zero), (zero, zero)), unroll=2
    )
    grad_out.go()
    rate_out.go()
    totals = jnp.concatenate(
        [jnp.transpose(columns_s[block * BLOCK : (block + 1) * BLOCK])[:2] for block in range(blocks)], axis=0
    )
    high = totals.astype(BF16)
    low_part = (totals - high.astype(F32)).astype(BF16)
    for block in range(blocks):
        mixed_out.buffer[block, BLOCK:, :LANES] = high
        mixed_out.buffer[block, BLOCK:, LANES:] = low_part
    mixed_out.go(slice(None), pl.ds(BLOCK, 2 * blocks))

    def vectors(part, lines):
        taps = jnp.sum(tap_sum_s[part], axis=1)[:KERNEL]
        stacked = jnp.concatenate([taps] + [one_row(line) for line in lines], axis=0)
        if part:
            stacked = stacked + turn(stacked)
        return jnp.transpose(
            jnp.concatenate([stacked, jnp.zeros((LANES - stacked.shape[0], LANES), F32)], axis=0)
        )

    vectors_out[:LANES] = vectors(0, (main_conv, main_gain, main_bias, main_up))
    vectors_out[LANES:] = vectors(1, (rest_conv, rest_gain, rest_bias, rest_up))[: channels - LANES]


def attend_back_kernel(
    cot_ref,
    merge_ref,
    head_ref,
    attn_ref,
    value_ref,
    prob_ref,
    key_ref,
    coarse_ref,
    fine_ref,
    pos_ref,
    query_ref,
    n_ref,
    q_position_ref,
    qkv_ref,
    hat_ref,
    gain_ref,
    early_ref,
    branch_out,
    total_out,
    pack_0,
    pack_1,
    pack_2,
    pack_3,
    lines_out,
    grad_s,
    raw_s,
    projected_s,
    parts_s,
    grads_s,
):
    place = lax.axis_index("tm")
    frames = raw_s.shape[0]
    blocks = frames // BLOCK
    half = D // 2
    zero = jnp.zeros((8, LANES), F32)
    cot_ref, merge_ref, head_ref, attn_ref = cot_ref(), merge_ref(), head_ref(), attn_ref()
    head_ref[HEAD:] = jnp.zeros((LANES - HEAD, D), BF16)
    begin(value_ref, prob_ref, key_ref, pos_ref)

    @pl.loop(0, frames // TALL, unroll=4)
    def _(block):
        rows = rows_of(block, TALL)
        branch = dot_nt(cot_ref[rows], merge_ref[...]).astype(BF16)
        branch_out.buffer[rows] = branch
        grad = (dot_nt(branch, head_ref[...]) * attn_ref[rows, HEAD : HEAD + 1]).astype(BF16).astype(F32)
        delta = jnp.sum(grad * attn_ref[rows], axis=1, keepdims=True)
        high = delta.astype(BF16).astype(F32)
        lane = lax.broadcasted_iota(jnp.int32, (TALL, LANES), 1)
        grad = jnp.where(lane == HEAD, -high, jnp.where(lane == HEAD + 1, high - delta, grad))
        grad_s[rows] = grad.astype(BF16)

    branch_out.go()
    value_ref, prob_ref = value_ref(), prob_ref()
    key_ref, pos_ref = key_ref(), pos_ref()
    begin(query_ref, n_ref, q_position_ref, qkv_ref, hat_ref, early_ref)

    def score_step(block, sums):
        content_sum, position_sum = sums
        rows = rows_of(block, TALL)
        grad = grad_s[rows]
        score = dot_nt(grad, value_ref[...])
        for part in range(TALL // 32):
            at = pl.ds(pl.multiple_of(block * TALL + part * 32, 32), 32)
            inner = slice(part * 32, part * 32 + 32)
            raw_s[at] = (prob_ref[at].astype(F32) * score[inner]).astype(BF16)
        query = dot_nn(raw_s[rows], key_ref[...]) * 0.125
        for part in range(TALL // 32):
            at = pl.ds(pl.multiple_of(block * TALL + part * 32, 32), 32)
            inner = part * 32 % BLOCK
            sine, cosine = angle_rows(
                coarse_ref, fine_ref, block * (TALL // BLOCK) + part * 32 // BLOCK, slice(inner, inner + 32)
            )
            inner = slice(part * 32, part * 32 + 32)
            first, second = query[inner, LANES : LANES + half], query[inner, LANES + half :]
            projected_s[at, :half] = (first * sine - second * cosine).astype(BF16)
            projected_s[at, half:] = (first * cosine + second * sine).astype(BF16)
        position = dot_nn(projected_s[rows], pos_ref[...])
        content = query[:, :LANES]
        parts_s[rows, :LANES] = (content + position).astype(BF16)
        return content_sum + fold_rows(content), position_sum + fold_rows(position)

    content_sum, position_sum = lax.fori_loop(0, frames // TALL, score_step, (zero, zero), unroll=4)
    query_ref, n_ref, q_position_ref = query_ref(), n_ref(), q_position_ref()
    qkv_ref, hat_ref = qkv_ref(), hat_ref()
    grad_key = dot_tn(query_ref[...], raw_s[...])
    grad_value = dot_tn(grad_s[...], prob_ref[...])
    for block in range(blocks):
        at = slice(block * BLOCK, (block + 1) * BLOCK)
        parts_s[at, LANES : 2 * LANES] = jnp.transpose(grad_key[:, at]).astype(BF16)
        parts_s[at, 2 * LANES :] = jnp.transpose(grad_value[:, at]).astype(BF16)
    grads_s[:HEAD] = dot_tn(parts_s[:, :LANES], n_ref[...])[:HEAD]
    grads_s[HEAD : 2 * HEAD] = dot_nn(grad_key.astype(BF16), n_ref[...])[:HEAD]
    grads_s[2 * HEAD : 3 * HEAD] = dot_nn(grad_value.astype(BF16), n_ref[...])[:HEAD]
    grads_s[3 * HEAD :] = dot_tn(q_position_ref[...], projected_s[...])[:HEAD]
    stream = lax.axis_index("stream")
    early_ref = early_ref()
    for apart, pack_out in enumerate((pack_0, pack_1, pack_2, pack_3)):
        quarter = lax.bitwise_xor(stream, jnp.int32(apart))
        lanes = pl.ds(pl.multiple_of(quarter * LANES, LANES), LANES)
        pack_out.buffer[: 4 * HEAD] = grads_s[:, lanes].astype(BF16)
        pack_out.buffer[4 * HEAD :] = early_ref[quarter]
        pack_out.go()
    gain = line_of(gain_ref)
    wide_zero = jnp.zeros((8, D), F32)

    def norm_step(block, sums):
        gain_sum, bias_sum = sums
        grad = dot_nt(parts_s[rows_of(block, TALL)], qkv_ref[...])
        for part in range(TALL // 32):
            at = pl.ds(pl.multiple_of(block * TALL + part * 32, 32), 32)
            own = grad[part * 32 : part * 32 + 32]
            total_out.buffer[at] = (own * gain).astype(BF16)
            gain_sum = gain_sum + fold_rows(own * hat_ref[at].astype(F32))
            bias_sum = bias_sum + fold_rows(own)
        return gain_sum, bias_sum

    gain_sum, bias_sum = lax.fori_loop(0, frames // TALL, norm_step, (wide_zero, wide_zero), unroll=4)
    lane = lax.broadcasted_iota(jnp.int32, (1, LANES), 1)

    def own_lanes(sums):
        line = one_row(sums)
        line = line + turn(line)
        tiles = [
            jnp.where(lax.div(tile * LANES + lane, HEAD) == place, line, 0.0) for tile in range(D // LANES)
        ]
        return jnp.concatenate(tiles, axis=1)

    lines_out[...] = jnp.concatenate(
        [
            one_row(gain_sum),
            one_row(bias_sum),
            own_lanes(content_sum),
            own_lanes(position_sum),
            jnp.zeros((4, D), F32),
        ],
        axis=0,
    )


def mlp_second_kernel(
    mixed_ref,
    gate_pre_ref,
    grad_ref,
    rate_ref,
    hat_ref,
    up_ref,
    norm_hat_ref,
    gain_ref,
    other_ref,
    pre_out,
    same_out,
    apart_out,
    lines_out,
    up_out,
    columns_s,
):
    place = lax.axis_index("tm")
    pre_s = pre_out.buffer
    frames = pre_s.shape[0]
    half = frames // 2
    blocks = frames // BLOCK
    totals = jnp.zeros((2 * blocks, LANES), F32)
    mixed_ref = mixed_ref()
    for source in range(mixed_ref.shape[0]):
        both = mixed_ref[source].astype(F32)
        totals = totals + (both[:, :LANES] + both[:, LANES:])
    totals = totals * (1.0 / HALF)
    high = totals.astype(BF16)
    low_part = (totals - high.astype(F32)).astype(BF16)
    both = jnp.concatenate([high, low_part], axis=0)
    lane = lax.broadcasted_iota(jnp.int32, (4 * blocks, 2 * LANES), 1) // LANES
    line = lax.broadcasted_iota(jnp.int32, (4 * blocks, 2 * LANES), 0)
    for block in range(blocks):
        chosen = (lax.rem(line, 2 * blocks) == 2 * block + lane).astype(F32).astype(BF16)
        columns_s[block * BLOCK : (block + 1) * BLOCK] = dot_tn(both, chosen)
    gate_pre_ref, grad_ref, rate_ref, hat_ref = gate_pre_ref(), grad_ref(), rate_ref(), hat_ref()
    begin(up_ref, norm_hat_ref, other_ref)
    low = low_lanes(64)
    gain = line_of(gain_ref)

    def chunk(start, base=0):
        return pl.ds(pl.multiple_of(start, 64) + base, 64)

    def pre_part(rows, table, up_sum):
        plain, along = table
        hat, rate = hat_ref[rows].astype(F32), rate_ref[rows].astype(F32)
        pre = (grad_ref[rows].astype(F32) - rate * (plain + hat * along)).astype(BF16).astype(F32)
        return pre, up_sum + fold_rows(pre)

    def pre_step(block, sums):
        main_up, rest_up = sums
        for part in range(TALL // 64):
            start = block * TALL + part * 64
            tables = []
            for base in (0, half):
                rows = chunk(start, base)
                table = [columns_s[rows, item * LANES : (item + 1) * LANES] for item in range(2)]
                tables.append(table)
                pre, main_up = pre_part(rows, table, main_up)
                pre_s[rows, :LANES] = gate_pre_ref[rows]
                pre_s[rows, 2 * LANES :] = pre.astype(BF16)
            rows = chunk(start, frames)
            table = [jnp.where(low, one, other) for one, other in zip(*tables)]
            pre, rest_up = pre_part(rows, table, rest_up)
            gate_pre = gate_pre_ref[rows].astype(F32)
            pre_s[chunk(start), LANES : 2 * LANES] = jnp.where(low, gate_pre, turn(pre)).astype(BF16)
            pre_s[chunk(start, half), LANES : 2 * LANES] = jnp.where(low, turn(gate_pre), pre).astype(BF16)
        return main_up, rest_up

    zero = jnp.zeros((8, LANES), F32)
    main_up, rest_up = lax.fori_loop(0, half // TALL, pre_step, (zero, zero), unroll=2)
    pre_out.go()
    up_ref, norm_hat_ref, other_ref = up_ref(), norm_hat_ref(), other_ref()
    wide_zero = jnp.zeros((8, D), F32)

    def norm_step(step, sums):
        gain_sum, bias_sum = sums
        grads = dot_nt(pre_s[rows_of(step, TALL)], up_ref[...])
        for part in range(TALL // BLOCK):
            block = step * (TALL // BLOCK) + part
            rows = rows_of(block, BLOCK)
            grad = grads[part * BLOCK : (part + 1) * BLOCK]
            total = (grad * gain + other_ref[rows].astype(F32)).astype(BF16)
            apart = lax.bitwise_xor(block, place)

            @pl.when(lax.rem(apart, 2) == 0)
            def _(apart=apart, total=total):
                same_out.buffer[lax.div(apart, 2)] = total

            @pl.when(lax.rem(apart, 2) == 1)
            def _(apart=apart, total=total):
                apart_out.buffer[lax.div(apart, 2)] = total

            gain_sum = gain_sum + fold_rows(grad * norm_hat_ref[rows].astype(F32))
            bias_sum = bias_sum + fold_rows(grad)
        return gain_sum, bias_sum

    gain_sum, bias_sum = lax.fori_loop(0, frames // TALL, norm_step, (wide_zero, wide_zero), unroll=2)
    apart_out.go()
    same_out.go()
    lines_out[...] = jnp.concatenate([one_row(gain_sum), one_row(bias_sum), jnp.zeros((6, D), F32)], axis=0)
    rest_line = one_row(rest_up)
    up_out[:LANES] = jnp.transpose(jnp.broadcast_to(one_row(main_up), (LANES, LANES)))
    up_out[LANES:] = jnp.transpose(jnp.broadcast_to(rest_line + turn(rest_line), (LANES, LANES)))[:LOW]


def late_pack_kernel(
    pre_ref,
    n_ref,
    joined_ref,
    branch_ref,
    cot_ref,
    vectors_ref,
    up_columns_ref,
    first_lines_ref,
    head_lines_ref,
    own_lines_ref,
    pack_out,
):
    pack_ref = pack_out.buffer
    quarters = pack_ref.shape[0]
    channels = vectors_ref.shape[0]
    share = channels // quarters
    gate_at = KERNEL + 3
    lane = lax.broadcasted_iota(jnp.int32, (share, LANES), 1)
    lines = jnp.concatenate(
        [
            head_lines_ref[0:2],
            own_lines_ref[0:2],
            head_lines_ref[2:4],
            first_lines_ref[0:2],
            jnp.zeros((8, D), F32),
        ],
        axis=0,
    )
    for quarter in range(quarters):
        table = vectors_ref[quarter * share : (quarter + 1) * share]
        for other in range(2):
            at = slice((2 * (quarter % 2) + other) * share, (2 * (quarter % 2) + other + 1) * share)
            column = vectors_ref[at, gate_at : gate_at + 1] if quarter < quarters // 2 else up_columns_ref[at, 0:1]
            table = jnp.where(lane == gate_at + other, column, table)
        pack_ref[quarter, channels : channels + share] = table.astype(BF16)
        pack_ref[quarter, channels + share : channels + share + 16] = lines[
            :, quarter * LANES : (quarter + 1) * LANES
        ].astype(BF16)
    pre_ref, n_ref = pre_ref(), n_ref()
    begin(joined_ref, branch_ref, cot_ref)
    grad_up = dot_tn(pre_ref[...], n_ref[...])
    for quarter in range(quarters):
        lanes = slice(quarter * LANES, (quarter + 1) * LANES)
        pack_ref[quarter, :LANES] = grad_up[LANES:, lanes].astype(BF16)
        pack_ref[quarter, LANES:channels] = grad_up[LOW:LANES, lanes].astype(BF16)
    joined_ref, cot_ref, branch_ref = joined_ref(), cot_ref(), branch_ref()
    sources, _, rows = joined_ref.shape
    merge_rows = 2 * D // sources
    head_rows = D // sources
    grad_merge = jnp.zeros((merge_rows, D), F32)
    grad_head = jnp.zeros((head_rows, D), F32)
    for source in range(sources):
        at = slice(source * rows, (source + 1) * rows)
        joined = joined_ref[source]
        grad_merge = grad_merge + dot_nn(joined[:merge_rows], cot_ref[at])
        grad_head = grad_head + dot_nn(joined[merge_rows : merge_rows + head_rows], branch_ref[at])
    for quarter in range(quarters):
        base = channels + share + 16
        for grad in (grad_merge, grad_head):
            part = grad.shape[0] // quarters
            for tile in range(4):
                pack_ref[quarter, base : base + part] = grad[
                    quarter * part : (quarter + 1) * part, tile * LANES : (tile + 1) * LANES
                ].astype(BF16)
                base += part


def output_kernel(
    x_ref, mixed_ref, head_ref, down_ref, down_bias_ref, merge_ref, merge_bias_ref, out_ref, joined_out
):
    sources = mixed_ref.shape[0]
    rows = x_ref.shape[0]
    channels = HALF // sources
    share = channels // 4
    attn_parts = []
    branch_attn = jnp.zeros((rows, D), F32)
    branch_mlp = jnp.zeros((rows, D), F32)
    for source in range(sources):
        attn = turn(mixed_ref[source, :rows, LANES:].astype(F32))[:, :HEAD].astype(BF16)
        attn_parts.append(attn)
        branch_attn = branch_attn + dot_nn(attn, head_ref[source * HEAD : (source + 1) * HEAD])
        down = jnp.concatenate(
            [down_ref[(part * sources + source) * share : (part * sources + source + 1) * share] for part in range(4)],
            axis=0,
        )
        branch_mlp = branch_mlp + dot_nn(mixed_ref[source, :rows, :channels], down)
    joined = jnp.concatenate(
        [branch_attn.astype(BF16), (branch_mlp + line_of(down_bias_ref)).astype(BF16)], axis=1
    )
    result = x_ref[...].astype(F32) + dot_nn(joined, merge_ref[...]) + line_of(merge_bias_ref)
    out_ref[...] = result.astype(BF16)
    turned = jnp.transpose(joined.astype(F32))
    heads = jnp.transpose(jnp.concatenate(attn_parts, axis=1).astype(F32))
    merge_share = turned.shape[0] // (4 * sources)
    head_share = heads.shape[0] // (4 * sources)
    used = 4 * (merge_share + head_share)
    for target in range(sources):
        for part in range(4):
            at = (part * sources + target) * merge_share
            joined_out[target, part * merge_share : (part + 1) * merge_share] = turned[
                at : at + merge_share
            ].astype(BF16)
            at = (part * sources + target) * head_share
            to = 4 * merge_share + part * head_share
            joined_out[target, to : to + head_share] = heads[at : at + head_share].astype(BF16)
        joined_out[target, used:] = jnp.zeros((joined_out.shape[1] - used, rows), BF16)


def pair_kernel(same_ref, other_ref, *out_refs):
    for slot, out_ref in enumerate(out_refs):
        out_ref[...] = (same_ref[slot].astype(F32) + other_ref[slot].astype(F32)).astype(BF16)


def frames_kernel(x_ref, cot_ref, *refs):
    total_refs, out_ref = refs[:-1], refs[-1]
    for part in range(x_ref.shape[0] // 32):
        rows = slice(part * 32, part * 32 + 32)
        inputs = x_ref[rows].astype(F32)
        mean = jnp.mean(inputs, axis=-1, keepdims=True)
        centred = inputs - mean
        rate = lax.rsqrt(jnp.mean(centred * centred, axis=-1, keepdims=True) + EPS)
        hat = centred * rate
        grad = total_refs[0][rows].astype(F32)
        for total_ref in total_refs[1:]:
            grad = grad + total_ref[rows].astype(F32)
        plain = jnp.mean(grad, axis=-1, keepdims=True)
        along = jnp.mean(grad * hat, axis=-1, keepdims=True)
        out_ref[rows] = cot_ref[rows].astype(F32) + rate * (grad - plain - hat * along)


def add_kernel(*refs):
    out_ref = refs[-1]
    first = 0
    for at in range(0, len(refs) - 1, 4):
        total = refs[at][...].astype(F32)
        for ref in refs[at + 1 : at + 4]:
            total = total + ref[...].astype(F32)
        out_ref[first : first + total.shape[0]] = total.astype(BF16)
        first += total.shape[0]


def gather_parts(near_ref, far_ref, all_s):
    place = lax.axis_index("tm")
    for apart in range(all_s.shape[0]):
        part_ref = far_ref if apart % 2 else near_ref
        all_s[lax.bitwise_xor(jnp.int32(apart), place)] = part_ref[apart // 2]


def lines_from(all_s, base, size):
    return jnp.concatenate([all_s[source, base : base + size] for source in range(all_s.shape[0])], axis=0).astype(F32)


def add_streams_kernel(parts_ref, out_ref):
    total = parts_ref[0].astype(F32)
    for source in range(1, parts_ref.shape[0]):
        total = total + parts_ref[source].astype(F32)
    out_ref[...] = total.astype(BF16)


def early_kernel(near_ref, far_ref, qkv_out, pos_out, down_out, up_out, all_s):
    gather_parts(near_ref, far_ref, all_s)
    sources = all_s.shape[0]
    share = HALF // (4 * sources)
    for kind in range(4):
        lines = jnp.transpose(lines_from(all_s, kind * HEAD, HEAD))
        if kind < 3:
            qkv_out[:, kind * D : (kind + 1) * D] = lines
        else:
            pos_out[...] = lines
    base = 4 * HEAD
    for source in range(sources):
        for tile in range(4):
            down_out[source * share : (source + 1) * share, tile * LANES : (tile + 1) * LANES] = all_s[
                source, base + tile * share : base + (tile + 1) * share
            ].astype(F32)
    wide = sources * share
    for group in range(4):
        up_out.buffer[:, group * wide : (group + 1) * wide] = jnp.transpose(
            lines_from(all_s, base + 4 * share + group * share, share)
        )


def late_kernel(*refs):
    _, near_ref, far_ref = refs[:3]
    (
        attn_gain_out,
        attn_bias_out,
        mlp_gain_out,
        mlp_bias_out,
        content_out,
        position_out,
        outw_out,
        up_out,
        up_bias_out,
        gain_out,
        bias_out,
        taps_out,
        conv_bias_out,
        down_bias_out,
        merge_out,
        merge_bias_out,
        all_s,
    ) = refs[3:]
    gather_parts(near_ref, far_ref, all_s)
    sources = all_s.shape[0]
    channels = HALF // sources
    share = channels // 4
    base = 0
    for group in range(4):
        at = group * sources * share
        up_out.buffer[:, at : at + sources * share] = jnp.transpose(lines_from(all_s, base + group * share, share))
    up_out.go()
    table = jnp.transpose(lines_from(all_s, base + channels, share))
    taps_out[...] = table[:KERNEL]
    conv_bias_out[...] = table[KERNEL]
    gain_out[...] = table[KERNEL + 1]
    bias_out[...] = table[KERNEL + 2]
    wide = sources * share
    up_bias_out[:wide] = table[KERNEL + 3]
    up_bias_out[wide:] = table[KERNEL + 4]
    base = base + channels + share
    lines = all_s[0, base : base + 16].astype(F32)
    for source in range(1, sources):
        lines = lines + all_s[source, base : base + 16].astype(F32)
    outs = (attn_gain_out, attn_bias_out, mlp_gain_out, mlp_bias_out, content_out, position_out, down_bias_out, merge_bias_out)
    for line, out in enumerate(outs):
        out[...] = lines[line]
    base = base + 16
    merge_share = 2 * D // (4 * sources)
    head_share = D // (4 * sources)
    for source in range(sources):
        for tile in range(4):
            lanes = slice(tile * LANES, (tile + 1) * LANES)
            at = base + tile * merge_share
            merge_out[source * merge_share : (source + 1) * merge_share, lanes] = all_s[
                source, at : at + merge_share
            ].astype(F32)
            at = base + 4 * merge_share + tile * head_share
            outw_out[source * head_share : (source + 1) * head_share, lanes] = all_s[
                source, at : at + head_share
            ].astype(F32)


def moved(block, axis, bits):
    count = lax.axis_size(axis)
    return lax.ppermute(block, axis, [(index, index ^ bits) for index in range(count)])


def over_streams(packs):
    return [packs[0]] + [moved(packs[bits], "stream", bits) for bits in range(1, lax.axis_size("stream"))]


def near_blocks(block):
    return [block] + [moved(block, "tm", bits) for bits in range(2, lax.axis_size("tm"), 2)]


def far_blocks(near):
    far = [moved(part, "tm", 1) for part in near]
    return [part for pair in zip(near, far) for part in pair]


def far_stack(near):
    stack = jnp.stack(near)
    return stack, moved(stack, "tm", 1)


def head_device(
    frames,
    lengths,
    cotangent,
    ln_attn_gain,
    ln_attn_bias,
    ln_mlp_gain,
    ln_mlp_bias,
    qkv_weight,
    content_bias,
    position_bias,
    pos_weight,
    out_weight,
    up_weight,
    up_bias,
    gate_norm_gain,
    gate_norm_bias,
    conv_kernel,
    conv_bias,
    down_weight,
    down_bias,
    merge_weight,
    merge_bias,
):
    count = lax.axis_size("tm")
    quarters = lax.axis_size("stream")
    own = frames.shape[1]
    total = own * count
    folded = total + total // 2
    padded = folded + 4 * MARGIN
    share = HALF // (quarters * count)
    channels = HALF // count
    quarter = D // quarters
    own_frames = frames[0]
    own_cotangent = cotangent[0]

    whole, late = Part(), Part(late=True)
    near = near_blocks(jnp.concatenate([own_frames, own_cotangent], axis=1))
    up_own, table, qkv_own, pos_own, bias_own = kernel_call(
        select_kernel,
        [
            ((D, 3 * LANES), BF16),
            ((2, 8 + KERNEL + 1, LANES), F32),
            ((D, 3 * LANES), BF16),
            ((D, LANES), BF16),
            ((8, LANES), F32),
        ],
        10 * "v",
    )(
        up_weight,
        up_bias,
        gate_norm_gain,
        gate_norm_bias,
        conv_bias,
        conv_kernel,
        qkv_weight,
        pos_weight,
        content_bias,
        position_bias,
    )
    frequency = jnp.exp(jnp.arange(D // 2, dtype=F32) * (-2.0 * math.log(10000.0) / D))
    coarse = jnp.arange(0, total, BLOCK, dtype=F32)[:, None] * frequency[None]
    fine = jnp.arange(BLOCK, dtype=F32)[:, None] * frequency[None]
    coarse_table = jnp.concatenate([jnp.sin(coarse), jnp.cos(coarse)], axis=1)
    fine_table = jnp.concatenate([jnp.sin(fine), jnp.cos(fine)], axis=1)
    near, up_own, coarse_table, fine_table = lax.optimization_barrier((near, up_own, coarse_table, fine_table))
    blocks = far_blocks(near)

    n_attn, n_mlp, hat, q_position, query, key, value, prob, attn, mean, rate = kernel_call(
        attend_kernel,
        [
            ((total, D), BF16, 1),
            ((total, D), BF16, 1),
            ((total, D), BF16, 1),
            ((total, LANES), BF16, 1),
            ((total, LANES), BF16, 1),
            ((total, LANES + D), BF16, 1),
            ((total, LANES), BF16, 1),
            ((total, total), BF16, 1),
            ((total, LANES), F32, 1),
            ((total, LANES), F32, 1),
            ((total, LANES), F32, 1),
        ],
        [
            "s",
            blocks_part(0),
            *"vvvvvvvvv",
            Part((D, HALF), lambda refs, buffer: [(refs[0].at[:, pl.ds(HALF, HALF)], buffer)], late=True),
            "v",
        ],
        [((total, LANES + D), BF16)],
        bounds=True,
    )(
        lengths,
        *blocks,
        ln_attn_gain,
        ln_attn_bias,
        ln_mlp_gain,
        ln_mlp_bias,
        qkv_own,
        pos_own,
        bias_own,
        coarse_table,
        fine_table,
        up_weight,
        up_bias,
    )

    def own_down(refs, buffer):
        place = lax.axis_index("tm")
        stride = HALF // quarters
        return [
            (
                refs[0].at[pl.ds(pl.multiple_of(part * stride + share * place, 16), share)],
                buffer.at[pl.ds(part * share, share)],
            )
            for part in range(quarters)
        ]

    mixed, gate_pre, grad_y, slope, gate_hat, early_pack, vectors, first_lines = kernel_call(
        mlp_first_kernel,
        [
            ((count, own + 16, 2 * LANES), BF16, 1),
            ((folded, LANES), BF16, 1),
            ((folded, LANES), BF16, 1),
            ((folded, LANES), BF16, 1),
            ((folded, LANES), BF16, 1),
            ((quarters, 8 * share, LANES), BF16, 1),
            ((channels, LANES), F32),
            ((8, D), F32),
        ],
        [
            "s",
            whole,
            "v",
            "v",
            whole,
            whole,
            blocks_part(1, late=True),
            rows_part(D, D, late=True),
            Part((2 * LANES, D), own_down, late=True),
            Part(late=True),
        ],
        [
            ((folded, LANES), F32),
            ((folded, LANES), F32),
            ((total, 2 * LANES), BF16),
            ((folded, LANES), F32),
            ((folded, LANES), F32),
            ((padded, LANES), F32),
            ((padded, LANES), F32),
            ((folded, LANES), F32),
            ((folded, LANES), F32),
            ((total, D), BF16),
            ((total, 2 * LANES), BF16),
            ((2, 32, 8, LANES), F32),
            ((2, 32, 8, LANES), F32),
            ((2, 32, 8, LANES), F32),
            ((total, LANES), F32),
            ((3, WINDOW + 2 * MARGIN, LANES), F32),
            ((3, WINDOW + 2 * MARGIN, LANES), F32),
        ],
        bounds=True,
    )(lengths, n_mlp, up_own, table, mean, rate, *blocks, merge_weight, down_weight, attn)
    mixed_own = lax.all_to_all(mixed, "tm", 0, 0, tiled=True)

    def own_head(refs, buffer):
        at = pl.ds(pl.multiple_of(lax.axis_index("tm") * HEAD, HEAD), HEAD)
        return [(refs[0].at[at], buffer.at[pl.ds(0, HEAD)])]

    branch, from_attn, *head_packs, head_lines = kernel_call(
        attend_back_kernel,
        [
            ((total, D), BF16, 1),
            ((total, D), BF16, 1),
            *([((4 * HEAD + 8 * share, LANES), BF16, 1)] * quarters),
            ((8, D), F32),
        ],
        [
            blocks_part(1),
            rows_part(0, D),
            Part((LANES, D), own_head),
            whole,
            late,
            late,
            late,
            "v",
            "v",
            late,
            late,
            late,
            late,
            late,
            late,
            "v",
            late,
        ],
        [
            ((total, LANES), BF16),
            ((total, total), BF16),
            ((total, D), BF16),
            ((total, 3 * LANES), BF16),
            ((4 * HEAD, D), F32),
        ],
    )(
        *blocks,
        merge_weight,
        out_weight,
        attn,
        value,
        prob,
        key,
        coarse_table,
        fine_table,
        pos_own,
        query,
        n_attn,
        q_position,
        qkv_own,
        hat,
        ln_attn_gain,
        early_pack,
    )
    head_parts = over_streams(head_packs)
    mixed_own, _ = lax.optimization_barrier((mixed_own, head_lines))
    out_rows, joined = kernel_call(
        output_kernel,
        [((own, D), BF16), ((count, 256, own), BF16)],
        "vvvvvvv",
        megas=24,
    )(own_frames, mixed_own, out_weight, down_weight, down_bias, merge_weight, merge_bias)
    joined_all = lax.all_to_all(joined, "tm", 0, 0, tiled=True)
    gate_pre, _ = lax.optimization_barrier((gate_pre, joined))
    late_rows = 5 * share + 16 + 3 * D // count
    pre, same, apart, own_lines, up_columns = kernel_call(
        mlp_second_kernel,
        [
            ((total, 3 * LANES), BF16, 1),
            ((count // 2, own, D), BF16, 1),
            ((count // 2, own, D), BF16, 1),
            ((8, D), F32),
            ((channels, LANES), F32),
        ],
        [
            Part(
                (count, 2 * total // BLOCK, 2 * LANES),
                lambda refs, buffer: [(refs[0].at[:, pl.ds(own, 2 * total // BLOCK)], buffer)],
            ),
            *([whole] * 4),
            late,
            late,
            "v",
            late,
        ],
        [((total, 2 * LANES), F32)],
    )(mixed_own, gate_pre, grad_y, slope, gate_hat, up_own, hat, ln_mlp_gain, from_attn)
    sibling = moved(apart, "tm", 1)
    pre, joined_all = lax.optimization_barrier((pre, joined_all))
    (late_pack,) = kernel_call(
        late_pack_kernel,
        [((quarters, late_rows, LANES), BF16, 1)],
        [
            Part(
                (total, 2 * LANES),
                lambda refs, buffer: [(refs[0].at[:, pl.ds(LANES, 2 * LANES)], buffer)],
            ),
            whole,
            late,
            late,
            blocks_part(1, late=True),
            *"vvvvv",
        ],
    )(pre, n_mlp, joined_all, branch, *blocks, vectors, up_columns, first_lines, head_lines, own_lines)
    late_pack, head_parts = lax.optimization_barrier((late_pack, head_parts))
    late_moved = lax.all_to_all(late_pack, "stream", 0, 0, tiled=True)
    (early_part,) = kernel_call(add_kernel, [((4 * HEAD + 8 * share, LANES), BF16)], quarters * "v", megas=24)(
        *head_parts
    )
    early_near = near_blocks(early_part)
    pairs = kernel_call(pair_kernel, [((own, D), BF16)] * (count // 2), "vv", megas=24)(same, sibling)
    sums = [pairs[0]] + [moved(pairs[slot], "tm", 2 * slot) for slot in range(1, count // 2)]
    late_moved, early_near, sums[1] = lax.optimization_barrier((late_moved, early_near, sums[1]))
    (late_part,) = kernel_call(add_streams_kernel, [((late_rows, LANES), BF16)], "v", megas=24)(late_moved)
    late_near = near_blocks(late_part)
    early_all = far_stack(early_near)
    grad_qkv, grad_pos, grad_down, half_up = kernel_call(
        early_kernel,
        [
            ((quarter, 3 * D), F32),
            ((quarter, D), F32),
            ((HALF // quarters, D), F32),
            ((quarter, 2 * HALF), F32, 1, (quarter, HALF), lambda ref: ref.at[:, pl.ds(0, HALF)]),
        ],
        "vv",
        [((count, 4 * HEAD + 8 * share, LANES), BF16)],
        megas=24,
    )(*early_all)
    late_near, grad_pos, sums = lax.optimization_barrier((late_near, grad_pos, sums))
    late_parts = far_stack(late_near)
    (grad_frames,) = kernel_call(frames_kernel, [((own, D), F32)], (2 + count // 2) * "v", megas=24)(
        own_frames, own_cotangent, *sums
    )
    late_parts, grad_frames = lax.optimization_barrier((late_parts, grad_frames))
    late = kernel_call(
        late_kernel,
        [((quarter,), F32)] * 6
        + [
            ((quarter, D), F32),
            ((quarter, 2 * HALF), F32, 1, (quarter, HALF), lambda ref: ref.at[:, pl.ds(HALF, HALF)]),
            ((2 * HALF // quarters,), F32),
            ((HALF // quarters,), F32),
            ((HALF // quarters,), F32),
            ((KERNEL, HALF // quarters), F32),
            ((HALF // quarters,), F32),
            ((quarter,), F32),
            ((2 * D // quarters, D), F32),
            ((quarter,), F32),
        ],
        "kvv",
        [((count,) + late_part.shape, BF16)],
        megas=24,
        aliases={0: 7},
    )(half_up, *late_parts)
    return (
        out_rows[None],
        grad_frames[None],
        *late[:4],
        grad_qkv,
        *late[4:6],
        grad_pos,
        *late[6:13],
        grad_down,
        *late[13:],
    )


def per_device(*operands):
    fits = (
        lax.axis_size("tm") == HEADS
        and lax.axis_size("stream") * LANES == D
        and operands[0].shape[1] == BLOCK
    )
    return head_device(*operands) if fits else frame_device(*operands)


def solution(mesh):
    return jax.shard_map(
        per_device,
        mesh=mesh,
        in_specs=(
            P("stream", "tm", None),
            P("stream", None),
            P("stream", "tm", None),
            P(),
            P(),
            P(),
            P(),
            P(),
            P(),
            P(),
            P(),
            P(),
            P(),
            P(),
            P(),
            P(),
            P(),
            P(),
            P(),
            P(),
            P(),
            P(),
        ),
        out_specs=(
            P("stream", "tm", None),
            P("stream", "tm", None),
            P("stream"),
            P("stream"),
            P("stream"),
            P("stream"),
            P("stream", None),
            P("stream"),
            P("stream"),
            P("stream", None),
            P("stream", None),
            P("stream", None),
            P("stream"),
            P("stream"),
            P("stream"),
            P(None, "stream"),
            P("stream"),
            P("stream", None),
            P("stream"),
            P("stream", None),
            P("stream"),
        ),
        check_vma=False,
    )
```

```python
import math

import jax
import jax.numpy as jnp
from jax import lax
from jax.experimental import pallas as pl
from jax.experimental.pallas import tpu as pltpu
from jax.sharding import PartitionSpec as P

D = 512
HEADS = 8
HEAD = 64
KERNEL = 31
ITEMS = 5
HALF = 1536


EPS = 1e-05
MASKED = -1e30


def extended(block, sides, width):
    for axis, dim in sides:
        count = lax.axis_size(axis)
        forward = [(i, i + 1) for i in range(count - 1)]
        backward = [(target, source) for source, target in forward]
        low = lax.ppermute(
            lax.slice_in_dim(block, block.shape[dim] - width, None, axis=dim), axis, forward
        )
        high = lax.ppermute(lax.slice_in_dim(block, 0, width, axis=dim), axis, backward)
        block = jnp.concatenate([low, block, high], axis=dim)
    return block


def norm_rows(inputs, scale_row, shift_row):
    row_mean = jnp.mean(inputs, axis=-1, keepdims=True)
    centred = inputs - row_mean
    spread = jnp.mean(centred * centred, axis=-1, keepdims=True)
    return centred * lax.rsqrt(spread + EPS) * scale_row + shift_row


def gelu_exact(inputs):
    return jax.nn.gelu(inputs, approximate=False)


def frame_info(lengths, offset, extent):
    item_ends = jnp.cumsum(lengths)
    first_table = jnp.concatenate([item_ends - lengths, item_ends[-1:]])
    frame_index = offset + jnp.arange(extent, dtype=jnp.int32)
    item_of = jnp.sum((frame_index[:, None] >= item_ends[None, :]).astype(jnp.int32), axis=1)
    labels = jnp.arange(ITEMS + 1, dtype=jnp.int32)
    first_frame = jnp.sum(
        jnp.where(item_of[:, None] == labels[None, :], first_table[None, :], 0), axis=1
    )
    return (frame_index, item_of, frame_index - first_frame)


def angles(place_in):
    frequency = jnp.exp(jnp.arange(D // 2, dtype=jnp.float32) * (-2.0 * math.log(10000.0) / D))
    phase_angle = place_in.astype(jnp.float32)[:, None] * frequency[None, :]
    return (jnp.sin(phase_angle), jnp.cos(phase_angle))


def rel_query(projected, sine_rows, cosine_rows):
    half_size = projected.shape[-1] // 2
    first_half = projected[..., :half_size]
    second_half = projected[..., half_size:]
    sine_wide = sine_rows[:, None, :]
    cosine_wide = cosine_rows[:, None, :]
    return jnp.concatenate(
        [
            first_half * sine_wide + second_half * cosine_wide,
            second_half * sine_wide - first_half * cosine_wide,
        ],
        axis=-1,
    )


def step_size(extent):
    return math.gcd(extent, 512)


def score_block(q_content, q_rel, query_item, query_frame, key_block, key_start, lengths):
    extent = key_block.shape[0]
    key_frame, key_item, key_place = frame_info(lengths, key_start, extent)
    sine_rows, cosine_rows = angles(key_place)
    k_rel = jnp.concatenate([cosine_rows, sine_rows], axis=1).astype(jnp.bfloat16)
    raw_scores = jnp.einsum(
        "qhe,khe->hqk",
        q_content,
        key_block.reshape(extent, HEADS, HEAD),
        preferred_element_type=jnp.float32,
    )
    raw_scores = raw_scores + jnp.einsum(
        "qhc,kc->hqk", q_rel, k_rel, preferred_element_type=jnp.float32
    )
    allowed = (query_item[:, None] == key_item[None, :]) & (
        (query_item[:, None] < ITEMS) | (query_frame[:, None] == key_frame[None, :])
    )
    return (raw_scores, allowed, k_rel)


def block_grads(
    q_content,
    q_rel,
    query_item,
    query_frame,
    grad_out,
    log_total,
    delta_rows,
    key_block,
    value_block,
    key_start,
    lengths,
):
    extent = key_block.shape[0]
    raw_scores, allowed, k_rel = score_block(
        q_content, q_rel, query_item, query_frame, key_block, key_start, lengths
    )
    prob_rows = jnp.where(allowed[None], jnp.exp(raw_scores * 0.125 - log_total[:, :, None]), 0.0)
    grad_prob = jnp.einsum(
        "qhe,khe->hqk",
        grad_out,
        value_block.reshape(extent, HEADS, HEAD),
        preferred_element_type=jnp.float32,
    )
    grad_raw = (prob_rows * (grad_prob - delta_rows[:, :, None]) * 0.125).astype(jnp.bfloat16)
    return (prob_rows.astype(jnp.bfloat16), grad_raw, k_rel)


def frame_device(
    frames,
    lengths,
    cotangent,
    ln_attn_gain,
    ln_attn_bias,
    ln_mlp_gain,
    ln_mlp_bias,
    qkv_weight,
    content_bias,
    position_bias,
    pos_weight,
    out_weight,
    up_weight,
    up_bias,
    gate_norm_gain,
    gate_norm_bias,
    conv_kernel,
    conv_bias,
    down_weight,
    down_bias,
    merge_weight,
    merge_bias,
):
    row_count = frames.shape[1]
    cycle_size = lax.axis_size("tm")
    offset = lax.axis_index("tm") * row_count
    stream_lengths = lengths[0]
    inputs = frames[0].astype(jnp.float32)
    frame_index, item_of, place_in = frame_info(stream_lengths, offset, row_count)
    sine_rows, cosine_rows = angles(place_in)
    attn_norm, attn_pull = jax.vjp(
        norm_rows, inputs, ln_attn_gain.astype(jnp.float32), ln_attn_bias.astype(jnp.float32)
    )
    mlp_norm, mlp_pull = jax.vjp(
        norm_rows, inputs, ln_mlp_gain.astype(jnp.float32), ln_mlp_bias.astype(jnp.float32)
    )
    attn_norm_low = attn_norm.astype(jnp.bfloat16)
    mlp_norm_low = mlp_norm.astype(jnp.bfloat16)
    qkv_rows = jnp.dot(attn_norm_low, qkv_weight, preferred_element_type=jnp.float32)
    query_rows = qkv_rows[:, :D]
    key_rows = qkv_rows[:, D : 2 * D].astype(jnp.bfloat16)
    value_rows = qkv_rows[:, 2 * D :].astype(jnp.bfloat16)
    q_content = (query_rows + content_bias.astype(jnp.float32)).astype(jnp.bfloat16)
    q_position = (query_rows + position_bias.astype(jnp.float32)).astype(jnp.bfloat16)
    content_heads = q_content.reshape(row_count, HEADS, HEAD)
    position_heads = q_position.reshape(row_count, HEADS, HEAD)
    pos_heads = pos_weight.reshape(D, HEADS, HEAD)
    projected = jnp.einsum(
        "the,che->thc", position_heads, pos_heads, preferred_element_type=jnp.float32
    )
    q_rel = rel_query(projected, sine_rows, cosine_rows).astype(jnp.bfloat16)
    start_state = (
        jnp.full((HEADS, row_count), MASKED, jnp.float32),
        jnp.zeros((HEADS, row_count), jnp.float32),
        jnp.zeros((HEADS, row_count, HEAD), jnp.float32),
    )
    fold_state = start_state
    key_piece = lax.all_gather(key_rows, "tm", axis=0, tiled=True)
    value_piece = lax.all_gather(value_rows, "tm", axis=0, tiled=True)
    extent = key_piece.shape[0]
    step_rows = step_size(extent)

    def forward_one_step(inner_state, step_index):
        row_top, row_total, row_acc = inner_state
        key_block = lax.dynamic_slice_in_dim(key_piece, step_index * step_rows, step_rows, 0)
        value_block = lax.dynamic_slice_in_dim(value_piece, step_index * step_rows, step_rows, 0)
        raw_scores, allowed, k_rel = score_block(
            content_heads,
            q_rel,
            item_of,
            frame_index,
            key_block,
            step_index * step_rows,
            stream_lengths,
        )
        scaled = jnp.where(allowed[None], raw_scores * 0.125, MASKED)
        new_top = jnp.maximum(row_top, jnp.max(scaled, axis=2))
        weight = jnp.where(allowed[None], jnp.exp(scaled - new_top[:, :, None]), 0.0)
        factor = jnp.exp(row_top - new_top)
        row_total = row_total * factor + jnp.sum(weight, axis=2)
        row_acc = row_acc * factor[:, :, None] + jnp.einsum(
            "hqk,khe->hqe",
            weight.astype(jnp.bfloat16),
            value_block.reshape(step_rows, HEADS, HEAD),
            preferred_element_type=jnp.float32,
        )
        return ((new_top, row_total, row_acc), None)

    fold_state, unused = lax.scan(
        forward_one_step, fold_state, jnp.arange(extent // step_rows, dtype=jnp.int32)
    )
    row_top, row_total, row_acc = fold_state
    attn_heads = row_acc / row_total[:, :, None]
    log_total = row_top + jnp.log(row_total)
    attn_low = jnp.transpose(attn_heads, (1, 0, 2)).reshape(row_count, D).astype(jnp.bfloat16)
    branch_attn = jnp.dot(attn_low, out_weight, preferred_element_type=jnp.float32).astype(
        jnp.bfloat16
    )
    hidden_pre = jnp.dot(
        mlp_norm_low, up_weight, preferred_element_type=jnp.float32
    ) + up_bias.astype(jnp.float32)
    hidden, gelu_pull = jax.vjp(gelu_exact, hidden_pre)
    gate_half = hidden[:, :HALF]
    conv_norm, conv_pull = jax.vjp(
        norm_rows,
        hidden[:, HALF:],
        gate_norm_gain.astype(jnp.float32),
        gate_norm_bias.astype(jnp.float32),
    )
    conv_in = conv_norm.astype(jnp.bfloat16)
    half_width = KERNEL // 2
    conv_wide = extended(conv_in, (("tm", 0),), half_width)
    wide_frame, wide_item, wide_place = frame_info(
        stream_lengths, offset - half_width, row_count + 2 * half_width
    )
    kernel_rows = conv_kernel.astype(jnp.float32)
    conv_out = conv_bias.astype(jnp.float32) + jnp.zeros_like(gate_half)
    for tap_index in range(KERNEL):
        same_item = (wide_item[tap_index : tap_index + row_count] == item_of)[:, None]
        conv_out = (
            conv_out
            + jnp.where(
                same_item, conv_wide[tap_index : tap_index + row_count].astype(jnp.float32), 0.0
            )
            * kernel_rows[tap_index]
        )
    gated_low = (gate_half * conv_out).astype(jnp.bfloat16)
    branch_mlp = (
        jnp.dot(gated_low, down_weight, preferred_element_type=jnp.float32)
        + down_bias.astype(jnp.float32)
    ).astype(jnp.bfloat16)
    joined = jnp.concatenate([branch_attn, branch_mlp], axis=1)
    result = (
        inputs
        + jnp.dot(joined, merge_weight, preferred_element_type=jnp.float32)
        + merge_bias.astype(jnp.float32)
    )
    out_rows = result.astype(jnp.bfloat16)[None]
    grad_low = cotangent[0]
    grad_rows = grad_low.astype(jnp.float32)
    grad_merge_bias = jnp.sum(grad_rows, axis=0)
    grad_merge_weight = jnp.einsum(
        "tc,td->cd", joined, grad_low, preferred_element_type=jnp.float32
    )
    grad_joined = jnp.einsum(
        "td,cd->tc", grad_low, merge_weight, preferred_element_type=jnp.float32
    )
    grad_attn_branch = grad_joined[:, :D].astype(jnp.bfloat16)
    grad_mlp_branch = grad_joined[:, D:].astype(jnp.bfloat16)
    grad_down_weight = jnp.einsum(
        "tc,td->cd", gated_low, grad_mlp_branch, preferred_element_type=jnp.float32
    )
    grad_down_bias = jnp.sum(grad_mlp_branch.astype(jnp.float32), axis=0)
    grad_gated = jnp.einsum(
        "td,cd->tc", grad_mlp_branch, down_weight, preferred_element_type=jnp.float32
    )
    grad_gate_half = grad_gated * conv_out
    grad_conv_out = (grad_gated * gate_half).astype(jnp.bfloat16)
    grad_conv_rows = grad_conv_out.astype(jnp.float32)
    grad_conv_bias = jnp.sum(grad_conv_rows, axis=0)
    grad_wide = extended(grad_conv_out, (("tm", 0),), half_width)
    kernel_list = []
    grad_conv_in = jnp.zeros_like(grad_conv_rows)
    for tap_index in range(KERNEL):
        same_item = (wide_item[tap_index : tap_index + row_count] == item_of)[:, None]
        kernel_list.append(
            jnp.sum(
                jnp.where(
                    same_item, conv_wide[tap_index : tap_index + row_count].astype(jnp.float32), 0.0
                )
                * grad_conv_rows,
                axis=0,
            )
        )
        back_start = 2 * half_width - tap_index
        back_item = (wide_item[back_start : back_start + row_count] == item_of)[:, None]
        grad_conv_in = (
            grad_conv_in
            + jnp.where(
                back_item, grad_wide[back_start : back_start + row_count].astype(jnp.float32), 0.0
            )
            * kernel_rows[tap_index]
        )
    grad_conv_kernel = jnp.stack(kernel_list)
    grad_second, grad_gate_norm_gain, grad_gate_norm_bias = conv_pull(grad_conv_in)
    (grad_pre_rows,) = gelu_pull(jnp.concatenate([grad_gate_half, grad_second], axis=1))
    grad_pre = grad_pre_rows.astype(jnp.bfloat16)
    grad_up_bias = jnp.sum(grad_pre.astype(jnp.float32), axis=0)
    grad_up_weight = jnp.einsum(
        "tc,tf->cf", mlp_norm_low, grad_pre, preferred_element_type=jnp.float32
    )
    grad_mlp_norm = jnp.einsum("tf,cf->tc", grad_pre, up_weight, preferred_element_type=jnp.float32)
    grad_out_weight = jnp.einsum(
        "tc,td->cd", attn_low, grad_attn_branch, preferred_element_type=jnp.float32
    )
    grad_attn_low = jnp.einsum(
        "td,cd->tc", grad_attn_branch, out_weight, preferred_element_type=jnp.float32
    ).astype(jnp.bfloat16)
    grad_out_heads = grad_attn_low.reshape(row_count, HEADS, HEAD)
    delta_rows = jnp.sum(
        jnp.transpose(grad_out_heads.astype(jnp.float32), (1, 0, 2)) * attn_heads, axis=2
    )
    total_frames = row_count * cycle_size
    back_start_state = (
        jnp.zeros((row_count, HEADS, HEAD), jnp.float32),
        jnp.zeros((row_count, HEADS, D), jnp.float32),
        jnp.zeros((total_frames, D), jnp.float32),
        jnp.zeros((total_frames, D), jnp.float32),
    )
    back_key_piece = lax.all_gather(key_rows, "tm", axis=0, tiled=True)
    back_value_piece = lax.all_gather(value_rows, "tm", axis=0, tiled=True)
    extent = back_key_piece.shape[0]
    back_step_rows = step_size(extent)

    def back_one_step(inner_state, step_index):
        grad_content, grad_rel = inner_state
        key_block = lax.dynamic_slice_in_dim(
            back_key_piece, step_index * back_step_rows, back_step_rows, 0
        )
        value_block = lax.dynamic_slice_in_dim(
            back_value_piece, step_index * back_step_rows, back_step_rows, 0
        )
        prob_low, grad_raw, k_rel = block_grads(
            content_heads,
            q_rel,
            item_of,
            frame_index,
            grad_out_heads,
            log_total,
            delta_rows,
            key_block,
            value_block,
            step_index * back_step_rows,
            stream_lengths,
        )
        grad_content = grad_content + jnp.einsum(
            "hqk,khe->qhe",
            grad_raw,
            key_block.reshape(back_step_rows, HEADS, HEAD),
            preferred_element_type=jnp.float32,
        )
        grad_rel = grad_rel + jnp.einsum(
            "hqk,kc->qhc", grad_raw, k_rel, preferred_element_type=jnp.float32
        )
        key_part = jnp.einsum(
            "hqk,qhe->khe", grad_raw, content_heads, preferred_element_type=jnp.float32
        ).reshape(back_step_rows, D)
        value_part = jnp.einsum(
            "hqk,qhe->khe", prob_low, grad_out_heads, preferred_element_type=jnp.float32
        ).reshape(back_step_rows, D)
        return ((grad_content, grad_rel), (key_part, value_part))

    inner_state, block_parts = lax.scan(
        back_one_step,
        (back_start_state[0], back_start_state[1]),
        jnp.arange(extent // back_step_rows, dtype=jnp.int32),
    )
    key_all = block_parts[0].reshape(extent, D)
    value_all = block_parts[1].reshape(extent, D)
    grad_content, grad_rel, key_all, value_all = (
        inner_state[0],
        inner_state[1],
        key_all,
        value_all,
    )
    grad_keys, grad_values = (
        lax.psum_scatter(key_all, "tm", scatter_dimension=0, tiled=True),
        lax.psum_scatter(value_all, "tm", scatter_dimension=0, tiled=True),
    )
    half_size = D // 2
    rel_first = grad_rel[..., :half_size]
    rel_second = grad_rel[..., half_size:]
    sine_wide = sine_rows[:, None, :]
    cosine_wide = cosine_rows[:, None, :]
    grad_projected = jnp.concatenate(
        [
            rel_first * sine_wide - rel_second * cosine_wide,
            rel_first * cosine_wide + rel_second * sine_wide,
        ],
        axis=-1,
    ).astype(jnp.bfloat16)
    grad_pos_weight = jnp.einsum(
        "thc,the->che", grad_projected, position_heads, preferred_element_type=jnp.float32
    ).reshape(D, D)
    grad_q_position = jnp.einsum(
        "thc,che->the", grad_projected, pos_heads, preferred_element_type=jnp.float32
    )
    grad_content_bias = jnp.sum(grad_content, axis=0).reshape(D)
    grad_position_bias = jnp.sum(grad_q_position, axis=0).reshape(D)
    grad_query = (grad_content + grad_q_position).reshape(row_count, D).astype(jnp.bfloat16)
    grad_qkv = jnp.concatenate(
        [grad_query, grad_keys.astype(jnp.bfloat16), grad_values.astype(jnp.bfloat16)], axis=1
    )
    grad_qkv_weight = jnp.einsum(
        "tc,tf->cf", attn_norm_low, grad_qkv, preferred_element_type=jnp.float32
    )
    grad_attn_norm = jnp.einsum(
        "tf,cf->tc", grad_qkv, qkv_weight, preferred_element_type=jnp.float32
    )
    grad_from_attn, grad_ln_attn_gain, grad_ln_attn_bias = attn_pull(grad_attn_norm)
    grad_from_mlp, grad_ln_mlp_gain, grad_ln_mlp_bias = mlp_pull(grad_mlp_norm)
    grad_inputs = grad_rows + grad_from_attn + grad_from_mlp
    weight_grads = (
        grad_ln_attn_gain,
        grad_ln_attn_bias,
        grad_ln_mlp_gain,
        grad_ln_mlp_bias,
        grad_qkv_weight,
        grad_content_bias,
        grad_position_bias,
        grad_pos_weight,
        grad_out_weight,
        grad_up_weight,
        grad_up_bias,
        grad_gate_norm_gain,
        grad_gate_norm_bias,
        grad_conv_kernel,
        grad_conv_bias,
        grad_down_weight,
        grad_down_bias,
        grad_merge_weight,
        grad_merge_bias,
    )
    summed = lax.psum(
        (
            weight_grads[0],
            weight_grads[1],
            weight_grads[2],
            weight_grads[3],
            weight_grads[4],
            weight_grads[5],
            weight_grads[6],
            weight_grads[7],
            weight_grads[8],
            weight_grads[9],
            weight_grads[10],
            weight_grads[11],
            weight_grads[12],
            weight_grads[13],
            weight_grads[14],
            weight_grads[15],
            weight_grads[16],
            weight_grads[17],
            weight_grads[18],
        ),
        "tm",
    )
    shares = (
        lax.psum_scatter(
            summed[0].astype(jnp.bfloat16), "stream", scatter_dimension=0, tiled=True
        ).astype(jnp.float32),
        lax.psum_scatter(
            summed[1].astype(jnp.bfloat16), "stream", scatter_dimension=0, tiled=True
        ).astype(jnp.float32),
        lax.psum_scatter(
            summed[2].astype(jnp.bfloat16), "stream", scatter_dimension=0, tiled=True
        ).astype(jnp.float32),
        lax.psum_scatter(
            summed[3].astype(jnp.bfloat16), "stream", scatter_dimension=0, tiled=True
        ).astype(jnp.float32),
        lax.psum_scatter(
            summed[4].astype(jnp.bfloat16), "stream", scatter_dimension=0, tiled=True
        ).astype(jnp.float32),
        lax.psum_scatter(
            summed[5].astype(jnp.bfloat16), "stream", scatter_dimension=0, tiled=True
        ).astype(jnp.float32),
        lax.psum_scatter(
            summed[6].astype(jnp.bfloat16), "stream", scatter_dimension=0, tiled=True
        ).astype(jnp.float32),
        lax.psum_scatter(
            summed[7].astype(jnp.bfloat16), "stream", scatter_dimension=0, tiled=True
        ).astype(jnp.float32),
        lax.psum_scatter(
            summed[8].astype(jnp.bfloat16), "stream", scatter_dimension=0, tiled=True
        ).astype(jnp.float32),
        lax.psum_scatter(
            summed[9].astype(jnp.bfloat16), "stream", scatter_dimension=0, tiled=True
        ).astype(jnp.float32),
        lax.psum_scatter(
            summed[10].astype(jnp.bfloat16), "stream", scatter_dimension=0, tiled=True
        ).astype(jnp.float32),
        lax.psum_scatter(
            summed[11].astype(jnp.bfloat16), "stream", scatter_dimension=0, tiled=True
        ).astype(jnp.float32),
        lax.psum_scatter(
            summed[12].astype(jnp.bfloat16), "stream", scatter_dimension=0, tiled=True
        ).astype(jnp.float32),
        lax.psum_scatter(
            summed[13].astype(jnp.bfloat16), "stream", scatter_dimension=1, tiled=True
        ).astype(jnp.float32),
        lax.psum_scatter(
            summed[14].astype(jnp.bfloat16), "stream", scatter_dimension=0, tiled=True
        ).astype(jnp.float32),
        lax.psum_scatter(
            summed[15].astype(jnp.bfloat16), "stream", scatter_dimension=0, tiled=True
        ).astype(jnp.float32),
        lax.psum_scatter(
            summed[16].astype(jnp.bfloat16), "stream", scatter_dimension=0, tiled=True
        ).astype(jnp.float32),
        lax.psum_scatter(
            summed[17].astype(jnp.bfloat16), "stream", scatter_dimension=0, tiled=True
        ).astype(jnp.float32),
        lax.psum_scatter(
            summed[18].astype(jnp.bfloat16), "stream", scatter_dimension=0, tiled=True
        ).astype(jnp.float32),
    )
    return (out_rows, grad_inputs[None]) + tuple(shares)


LANES = 128
LOW = LANES // 2
BLOCK = 128
TALL = 256
WINDOW = 64
MARGIN = 16
BOUNDS = 16
MEGA = 1024 * 1024
F32 = jnp.float32
BF16 = jnp.bfloat16


def dot_nn(left, right):
    return jnp.dot(left, right, preferred_element_type=F32)


def dot_nt(left, right):
    return lax.dot_general(left, right, (((1,), (1,)), ((), ())), preferred_element_type=F32)


def dot_tn(left, right):
    return lax.dot_general(left, right, (((0,), (0,)), ((), ())), preferred_element_type=F32)


def rows_of(index, size, base=0):
    return pl.ds(pl.multiple_of(index * size, size) + base, size)


def line_of(ref):
    return ref[...].astype(F32).reshape(1, ref.shape[0])


def fold_rows(values):
    return jnp.sum(values.reshape(values.shape[0] // 8, 8, values.shape[1]), axis=0)


def one_row(values):
    return jnp.sum(values, axis=0, keepdims=True)


def turn(values):
    return pltpu.roll(values, LOW, 1)


def low_lanes(rows):
    return lax.broadcasted_iota(jnp.int32, (rows, LANES), 1) < LOW


def centre_rows(inputs):
    mean = jnp.mean(inputs, axis=-1, keepdims=True)
    centred = inputs - mean
    spread = jnp.mean(centred * centred, axis=-1, keepdims=True)
    return centred * lax.rsqrt(spread + EPS)


def gelu_parts(values):
    phi = 0.5 + 0.5 * lax.erf(values * math.sqrt(0.5))
    bell = jnp.exp(values * values * -0.5)
    return values * phi, phi + values * bell * (1.0 / math.sqrt(2.0 * math.pi))


class Part:
    def __init__(self, shape=None, pairs=None, refs=1, late=False):
        self.shape, self.pairs, self.refs, self.late = shape, pairs, refs, late

    def buffer(self, operand):
        return self.shape or operand.shape

    def copies(self, refs, buffer):
        return self.pairs(refs, buffer) if self.pairs else [(refs[0], buffer)]


def blocks_part(half, late=False):
    def pairs(refs, buffer):
        place = lax.axis_index("tm")
        return [
            (
                ref.at[:, pl.ds(half * D, D)],
                buffer.at[rows_of(lax.bitwise_xor(jnp.int32(apart), place), BLOCK)],
            )
            for apart, ref in enumerate(refs)
        ]

    return Part((HEADS * BLOCK, D), pairs, HEADS, late)


def rows_part(first, size, late=False):
    return Part((size, D), lambda refs, buffer: [(refs[0].at[pl.ds(first, size)], buffer)], late=late)


class Fetch:
    def __init__(self, pairs, buffer, sems, first):
        self.buffer, self.begun = buffer, False
        self.pending = [
            pltpu.make_async_copy(source, target, sems.at[first + index])
            for index, (source, target) in enumerate(pairs)
        ]

    def begin(self):
        if not self.begun:
            for copy in self.pending:
                copy.start()
        self.begun = True

    def __call__(self):
        self.begin()
        for copy in self.pending:
            copy.wait()
        self.pending = []
        return self.buffer


def begin(*fetches):
    for fetch in fetches:
        fetch.begin()


class Send:
    def __init__(self, buffer, target, sems):
        self.buffer, self.target, self.sems, self.copies = buffer, target, sems, []

    def go(self, *index):
        source, target = (self.buffer.at[index], self.target.at[index]) if index else (self.buffer, self.target)
        copy = pltpu.make_async_copy(source, target, self.sems[len(self.copies)])
        copy.start()
        self.copies.append(copy)

    def finish(self):
        if not self.copies:
            self.go()


SPACES = {"v": pltpu.VMEM, "s": pltpu.SMEM, "k": pl.ANY}


def kernel_call(body, out_shapes, plan, scratch=(), megas=58, bounds=False, aliases=None):
    def call(*operands):
        in_specs, buffers, at = [], [], 0
        for item in plan:
            if item == "f":
                in_specs.append(pl.BlockSpec(memory_space=pl.ANY))
                buffers.append(pltpu.VMEM(operands[at].shape, operands[at].dtype))
                at += 1
            elif isinstance(item, Part):
                in_specs += [pl.BlockSpec(memory_space=pl.ANY)] * item.refs
                buffers.append(pltpu.VMEM(item.buffer(operands[at]), operands[at].dtype))
                at += item.refs
            else:
                in_specs.append(pl.BlockSpec(memory_space=SPACES[item]))
                at += 1
        sent = [out for out in out_shapes if len(out) > 2]
        buffers += [pltpu.VMEM(out[3] if len(out) > 3 else out[0], out[1]) for out in sent]
        sem_count = 96
        extra = [pltpu.SMEM((BOUNDS,), jnp.int32)] if bounds else []

        def outer(*refs):
            inputs, rest = refs[: len(in_specs)], refs[len(in_specs) :]
            outputs, rest = rest[: len(out_shapes)], rest[len(out_shapes) :]
            held, rest = list(rest[: len(buffers)]), rest[len(buffers) :]
            sems, rest = rest[0], rest[1:]
            given, at, used = [], 0, 0
            for item in plan:
                if item == "f":
                    given.append(Fetch([(inputs[at], held[0])], held.pop(0), sems, used))
                    given[-1].begin()
                    used += 1
                    at += 1
                elif isinstance(item, Part):
                    buffer = held.pop(0)
                    pairs = item.copies(inputs[at : at + item.refs], buffer)
                    given.append(Fetch(pairs, buffer, sems, used))
                    if not item.late:
                        given[-1].begin()
                    used += len(pairs)
                    at += item.refs
                else:
                    given.append(inputs[at])
                    at += 1
            results = []
            for out, ref in zip(out_shapes, outputs):
                if len(out) > 2:
                    target = out[4](ref) if len(out) > 3 else ref
                    results.append(Send(held.pop(0), target, [sems.at[used + index] for index in range(4)]))
                    used += 4
                else:
                    results.append(ref)
            assert used <= sem_count
            given = [item() if kind == "f" else item for kind, item in zip(plan, given)]
            body(*given, *results, *rest)
            for item in given:
                if isinstance(item, Fetch):
                    item()
            sends = [item for item in results if isinstance(item, Send)]
            for item in sends:
                item.finish()
            for item in sends:
                for copy in item.copies:
                    copy.wait()

        return pl.pallas_call(
            outer,
            out_shape=[jax.ShapeDtypeStruct(out[0], out[1]) for out in out_shapes],
            in_specs=in_specs,
            out_specs=[pl.BlockSpec(memory_space=pl.ANY if len(out) > 2 else pltpu.VMEM) for out in out_shapes],
            scratch_shapes=buffers
            + [pltpu.SemaphoreType.DMA((sem_count,))]
            + [pltpu.VMEM(shape, kind) for shape, kind in scratch]
            + extra,
            input_output_aliases=aliases or {},
            compiler_params=pltpu.CompilerParams(vmem_limit_bytes=megas * MEGA),
            cost_estimate=pl.CostEstimate(flops=0, bytes_accessed=0, transcendentals=0),
        )(*operands)

    return call


def fill_bounds(lengths_ref, bounds_s, total):
    bounds_s[0] = jnp.int32(0)
    end = jnp.int32(0)
    for item in range(ITEMS):
        end = end + lengths_ref[0, item]
        bounds_s[item + 1] = end
    for item in range(ITEMS + 1, BOUNDS):
        bounds_s[item] = jnp.int32(total)


def select_kernel(
    up_ref,
    up_bias_ref,
    gain_ref,
    bias_ref,
    conv_bias_ref,
    taps_ref,
    qkv_ref,
    pos_ref,
    content_ref,
    position_ref,
    up_out,
    table_out,
    qkv_out,
    pos_out,
    bias_out,
):
    place = lax.axis_index("tm")
    quarters = lax.axis_size("stream")
    share = HALF // (quarters * lax.axis_size("tm"))
    lane = lax.broadcasted_iota(jnp.int32, (1, 2 * LANES), 1)
    channel = jnp.where(lane < LANES + LOW, lane, lane - LOW)
    group = jnp.zeros_like(channel)
    for quarter in range(1, quarters):
        group = group + (channel >= quarter * share).astype(jnp.int32)
    source = group * (HALF // quarters) + share * place + channel - group * share
    chosen = (lax.broadcasted_iota(jnp.int32, (HALF, 2 * LANES), 0) == source).astype(F32).astype(BF16)
    gate = dot_nn(up_ref[:, :HALF], chosen)
    conv = dot_nn(up_ref[:, HALF:], chosen)
    up_out[:, :LANES] = gate[:, :LANES].astype(BF16)
    up_out[:, LANES : 2 * LANES] = jnp.where(low_lanes(D), gate[:, LANES:], conv[:, LANES:]).astype(BF16)
    up_out[:, 2 * LANES :] = conv[:, :LANES].astype(BF16)
    up_bias = line_of(up_bias_ref)
    lines = jnp.concatenate(
        [
            up_bias[:, :HALF],
            up_bias[:, HALF:],
            line_of(gain_ref),
            line_of(bias_ref),
            line_of(conv_bias_ref),
            jnp.zeros((3, HALF), F32),
        ],
        axis=0,
    )
    lines = dot_nn(lines.astype(BF16), chosen)
    taps = dot_nn(taps_ref[...], chosen)
    for part in range(2):
        lanes = slice(part * LANES, (part + 1) * LANES)
        table_out[part, :8] = lines[:, lanes]
        table_out[part, 8 : 8 + KERNEL] = taps[:, lanes]
        table_out[part, 8 + KERNEL :] = jnp.zeros((1, LANES), F32)

    odd = lax.rem(place, 2) == 1

    def head_lanes(ref, base):
        at = pl.ds(pl.multiple_of(lax.div(place, 2) * LANES + base, LANES), LANES)
        values = ref[:, at].astype(F32)
        values = jnp.where(odd, turn(values), values)
        return jnp.where(low_lanes(values.shape[0]), values, 0.0)

    for part in range(3):
        qkv_out[:, part * LANES : (part + 1) * LANES] = head_lanes(qkv_ref, part * D).astype(BF16)
    pos_out[...] = head_lanes(pos_ref, 0).astype(BF16)
    bias_out[...] = jnp.zeros((8, LANES), F32)
    for line, ref in enumerate((content_ref, position_ref)):
        values = line_of(ref)
        picked = values[:, :LANES]
        for tile in range(1, D // LANES):
            picked = jnp.where(
                lax.div(place, 2) == tile, values[:, tile * LANES : (tile + 1) * LANES], picked
            )
        picked = jnp.where(odd, turn(picked), picked)
        bias_out[line : line + 1] = jnp.where(low_lanes(1), picked, 0.0)


def angle_rows(coarse_ref, fine_ref, block, rows):
    half = D // 2
    base = coarse_ref[pl.ds(block, 1)]
    base_sine, base_cosine = base[:, :half], base[:, half:]
    sine, cosine = fine_ref[rows, :half], fine_ref[rows, half:]
    return base_sine * cosine + base_cosine * sine, base_cosine * cosine - base_sine * sine


def item_codes(bounds_s, index):
    code = jnp.zeros_like(index)
    for item in range(1, ITEMS + 1):
        code = code + (index >= bounds_s[item]).astype(jnp.int32)
    return jnp.where(code < ITEMS, code, ITEMS + index)


def attend_kernel(
    lengths_ref,
    x_ref,
    attn_gain_ref,
    attn_bias_ref,
    mlp_gain_ref,
    mlp_bias_ref,
    qkv_ref,
    pos_ref,
    bias_ref,
    coarse_ref,
    fine_ref,
    up_ref,
    up_bias_ref,
    n_attn_out,
    n_mlp_out,
    hat_out,
    q_position_out,
    query_out,
    key_out,
    value_out,
    prob_out,
    attn_out,
    mean_out,
    rate_out,
    bounds_s,
):
    frames = n_attn_out.buffer.shape[0]
    half = D // 2
    fill_bounds(lengths_ref, bounds_s, frames)
    attn_gain, attn_bias = line_of(attn_gain_ref), line_of(attn_bias_ref)
    mlp_gain, mlp_bias = line_of(mlp_gain_ref), line_of(mlp_bias_ref)
    content, position = bias_ref[0:1], bias_ref[1:2]
    x_ref = x_ref()
    begin(up_ref)
    lane = lax.broadcasted_iota(jnp.int32, (1, LANES), 1)
    spare = ((lane == HEAD) | (lane == HEAD + 1)).astype(F32)

    @pl.loop(0, frames // TALL, unroll=4)
    def _(block):
        rows = rows_of(block, TALL)
        for part in range(TALL // 32):
            at = pl.ds(pl.multiple_of(block * TALL + part * 32, 32), 32)
            hat = centre_rows(x_ref[at].astype(F32))
            hat_out.buffer[at] = hat.astype(BF16)
            n_attn_out.buffer[at] = (hat * attn_gain + attn_bias).astype(BF16)
            n_mlp_out.buffer[at] = (hat * mlp_gain + mlp_bias).astype(BF16)
        parts = dot_nn(n_attn_out.buffer[rows], qkv_ref[...])
        query = parts[:, :LANES]
        query_out.buffer[rows, :LANES] = ((query + content).astype(BF16).astype(F32) * 0.125).astype(BF16)
        q_position = (query + position).astype(BF16)
        q_position_out.buffer[rows] = q_position
        key_out.buffer[rows, :LANES] = parts[:, LANES : 2 * LANES].astype(BF16)
        value_out.buffer[rows] = (parts[:, 2 * LANES :] + spare).astype(BF16)
        projected = dot_nt(q_position, pos_ref[...])
        for part in range(TALL // 32):
            at = pl.ds(pl.multiple_of(block * TALL + part * 32, 32), 32)
            inner = part * 32 % BLOCK
            sine, cosine = angle_rows(
                coarse_ref, fine_ref, block * (TALL // BLOCK) + part * 32 // BLOCK, slice(inner, inner + 32)
            )
            first = projected[part * 32 : part * 32 + 32, :half]
            second = projected[part * 32 : part * 32 + 32, half:]
            query_out.buffer[at, LANES : LANES + half] = ((first * sine + second * cosine) * 0.125).astype(BF16)
            query_out.buffer[at, LANES + half :] = ((second * sine - first * cosine) * 0.125).astype(BF16)
            key_out.buffer[at, LANES : LANES + half] = cosine.astype(BF16)
            key_out.buffer[at, LANES + half :] = sine.astype(BF16)

    for out in (n_attn_out, n_mlp_out, hat_out, q_position_out, query_out, key_out, value_out):
        out.go()
    up_ref = up_ref()
    up_bias = line_of(up_bias_ref)[:, HALF:]
    @pl.loop(0, frames // TALL, unroll=2)
    def _(block):
        values = dot_nn(n_mlp_out.buffer[rows_of(block, TALL)], up_ref[...])
        for part in range(TALL // 16):
            pre = values[part * 16 : part * 16 + 16] + up_bias
            hidden = pre * (0.5 + 0.5 * lax.erf(pre * math.sqrt(0.5)))
            mean = jnp.mean(hidden, axis=-1, keepdims=True)
            centred = hidden - mean
            rate = lax.rsqrt(jnp.mean(centred * centred, axis=-1, keepdims=True) + EPS)
            at = pl.ds(pl.multiple_of(block * TALL + part * 16, 16), 16)
            mean_out.buffer[at] = jnp.broadcast_to(mean, (16, LANES))
            rate_out.buffer[at] = jnp.broadcast_to(rate, (16, LANES))

    mean_out.go()
    rate_out.go()
    key_code = item_codes(bounds_s, lax.broadcasted_iota(jnp.int32, (1, frames), 1))

    low = low_lanes(32)
    for block in range(frames // TALL):
        rows = pl.ds(block * TALL, TALL)
        raw = dot_nt(query_out.buffer[rows], key_out.buffer[...])
        for part in range(TALL // 32):
            start = block * TALL + part * 32
            index = start + lax.broadcasted_iota(jnp.int32, (32, 1), 0)
            scaled = jnp.where(
                item_codes(bounds_s, index) == key_code, raw[part * 32 : part * 32 + 32], MASKED
            )
            weight = jnp.exp(scaled - jnp.max(scaled, axis=1, keepdims=True))
            prob_out.buffer[pl.ds(start, 32)] = weight.astype(BF16)
        prob_out.go(rows)
        attn = dot_nn(prob_out.buffer[rows], value_out.buffer[...])
        for part in range(TALL // 32):
            own = attn[part * 32 : part * 32 + 32]
            share = 1.0 / own[:, HEAD : HEAD + 1]
            attn_out.buffer[pl.ds(block * TALL + part * 32, 32)] = jnp.where(low, own * share, share)


def fill_margins(wide_s, frames):
    edge = jnp.zeros((MARGIN, LANES), F32)
    wide_s[:MARGIN] = edge
    wide_s[MARGIN + frames : 2 * MARGIN + frames] = edge
    base = frames + 3 * MARGIN
    after = base + frames // 2
    low = low_lanes(MARGIN)
    wide_s[base - MARGIN : base] = jnp.where(low, 0.0, turn(wide_s[after - MARGIN : after]))
    wide_s[after : after + MARGIN] = jnp.where(low, turn(wide_s[base : base + MARGIN]), 0.0)


def item_span(bounds_s, frame):
    begin, end = bounds_s[0], bounds_s[BOUNDS - 1]
    for item in range(1, ITEMS + 1):
        edge = bounds_s[item]
        begin = jnp.where(frame >= edge, edge, begin)
    for item in range(ITEMS, 0, -1):
        edge = bounds_s[item]
        end = jnp.where(frame < edge, edge, end)
    return begin, end


def is_whole(bounds_s, start):
    begin, end = item_span(bounds_s, start)
    reach = KERNEL // 2
    low = (begin == 0) | (begin <= start - reach)
    high = (end == bounds_s[BOUNDS - 1]) | (end >= start + WINDOW + reach)
    return low & high & (end >= start + WINDOW)


def tap_limits(bounds_s, start):
    frame = start + lax.broadcasted_iota(jnp.int32, (WINDOW, LANES), 0)
    begin, end = item_span(bounds_s, frame)
    return begin - frame, end - frame


def grouped(values):
    return values.reshape(WINDOW // 8, 8, LANES)


def triple_places(step, frames):
    half = frames // 2
    return (
        pl.multiple_of(step * WINDOW, 2 * MARGIN),
        pl.multiple_of(step * WINDOW + half, 2 * MARGIN),
        pl.multiple_of(step * WINDOW + frames + 2 * MARGIN, 2 * MARGIN),
    )


def over_windows(bounds_s, frames, body):
    half = frames // 2

    @pl.loop(0, half // WINDOW)
    def _(step):
        start = step * WINDOW
        whole = is_whole(bounds_s, start) & is_whole(bounds_s, start + half)

        @pl.when(whole)
        def _():
            body(step, None)

        @pl.when(jnp.logical_not(whole))
        def _():
            first, second = tap_limits(bounds_s, start), tap_limits(bounds_s, start + half)
            low = low_lanes(WINDOW)
            rest = [jnp.where(low, one, other) for one, other in zip(first, second)]
            body(step, (first, second, rest))


def tap_mask(tap, limits):
    shift = tap - KERNEL // 2
    return None if limits is None else (limits[0] <= shift) & (limits[1] > shift)


def tap_view(window_ref, tap, mask):
    view = window_ref[tap + 1 : tap + 1 + WINDOW]
    return grouped(view if mask is None else jnp.where(mask, view, 0.0))


def mlp_first_kernel(
    lengths_ref,
    n_ref,
    up_ref,
    table_ref,
    mean_ref,
    rate_ref,
    cot_ref,
    merge_ref,
    down_ref,
    attn_ref,
    mixed_out,
    gate_pre_out,
    grad_out,
    rate_out,
    hat_out,
    early_out,
    vectors_out,
    lines_out,
    hat_s,
    slope_s,
    gate_s,
    hidden_s,
    gate_slope_s,
    conv_s,
    grad_s,
    out_s,
    back_s,
    branch_s,
    mix_s,
    taps_s,
    turn_s,
    tap_sum_s,
    columns_s,
    forward_s,
    backward_s,
    bounds_s,
):
    place = lax.axis_index("tm")
    frames = mix_s.shape[0]
    half = frames // 2
    blocks = frames // BLOCK
    quarters, early_rows, _ = early_out.buffer.shape
    share = early_rows // 8
    channels = quarters * share
    fill_bounds(lengths_ref, bounds_s, frames)
    for part in range(2):
        for tap in range(KERNEL):
            line = jnp.broadcast_to(table_ref[part, 8 + tap : 9 + tap], (8, LANES))
            taps_s[part, tap] = line
            turn_s[part, KERNEL - 1 - tap] = line
    tap_sum_s[...] = jnp.zeros(tap_sum_s.shape, F32)
    main, rest = table_ref[0, :8], table_ref[1, :8]
    mixed_bias = jnp.where(low_lanes(1), rest[0:1], rest[1:2])
    low = low_lanes(64)
    gate_pre_ref = gate_pre_out.buffer
    n_ref = n_ref()
    mean_ref, rate_ref = mean_ref(), rate_ref()
    begin(cot_ref, merge_ref, down_ref, attn_ref)

    def stat_rows(rows):
        return mean_ref[rows], rate_ref[rows]

    def chunk(start, base=0):
        return pl.ds(pl.multiple_of(start, 64) + base, 64)

    def conv_part(hidden, mean, rate, lines, rows, to_rows):
        hat = (hidden - mean) * rate
        hat_s[rows] = hat
        hat_out.buffer[rows] = hat.astype(BF16)
        conv_s[to_rows] = (hat * lines[2:3] + lines[3:4]).astype(BF16).astype(F32)

    @pl.loop(0, half // TALL, unroll=2)
    def _(block):
        pre = [dot_nn(n_ref[rows_of(block, TALL, base)], up_ref[...]) for base in (0, half)]
        for part in range(TALL // 64):
            inner = slice(part * 64, part * 64 + 64)
            start = block * TALL + part * 64
            mixed = []
            for values, base in zip(pre, (0, half)):
                rows = chunk(start, base)
                gate, gate_slope = gelu_parts(values[inner, :LANES] + main[0:1])
                hidden_s[rows] = gate
                gate_slope_s[rows] = gate_slope
                hidden, slope = gelu_parts(values[inner, 2 * LANES :] + main[1:2])
                mean, rate = stat_rows(rows)
                slope_s[rows] = slope * rate
                conv_part(hidden, mean, rate, main, rows, chunk(start, base + MARGIN))
                mixed.append((*gelu_parts(values[inner, LANES : 2 * LANES] + mixed_bias), mean, rate))
            (low_hidden, low_slope, low_mean, low_rate), (high_hidden, high_slope, high_mean, high_rate) = mixed
            rows = chunk(start, frames)
            hidden_s[rows] = jnp.where(low, low_hidden, turn(high_hidden))
            gate_slope_s[rows] = jnp.where(low, low_slope, turn(high_slope))
            rate = jnp.where(low, low_rate, high_rate)
            slope_s[rows] = jnp.where(low, turn(low_slope), high_slope) * rate
            conv_part(
                jnp.where(low, turn(low_hidden), high_hidden),
                jnp.where(low, low_mean, high_mean),
                rate,
                rest,
                rows,
                chunk(start, frames + 3 * MARGIN),
            )

    hat_out.go()
    fill_margins(conv_s, frames)
    tall = WINDOW + 2 * MARGIN
    outs = (0, half, frames)

    def convolve(step, limits):
        for index, base in enumerate(triple_places(step, frames)):
            forward_s[index] = conv_s[pl.ds(base, tall)]
        for index in range(3):
            own = None if limits is None else limits[index]
            total = jnp.zeros((WINDOW // 8, 8, LANES), F32)
            for tap in range(KERNEL):
                mask = tap_mask(tap, own)
                total = total + tap_view(forward_s.at[index], tap, mask) * taps_s[index // 2, tap][None]
            lines = rest if index == 2 else main
            out_s[rows_of(step, WINDOW, outs[index])] = total.reshape(WINDOW, LANES) + lines[4:5]

    over_windows(bounds_s, frames, convolve)
    cot_ref = cot_ref()
    merge_ref = merge_ref()
    down_ref = down_ref()
    attn_ref = attn_ref()
    down_ref[channels:] = jnp.zeros((2 * LANES - channels, D), BF16)
    zero = jnp.zeros((8, LANES), F32)

    def branch_part(grad_gated, rows, to_rows, sums):
        up_sum, conv_sum = sums
        gate, conv = hidden_s[rows], out_s[rows]
        gate_pre = (grad_gated * conv * gate_slope_s[rows]).astype(BF16)
        gate_pre_ref[rows] = gate_pre
        grad_conv = (grad_gated * gate).astype(BF16).astype(F32)
        grad_s[to_rows] = grad_conv
        gate_pre = gate_pre.astype(F32)
        return gate * conv, gate_pre, (up_sum + fold_rows(gate_pre), conv_sum + fold_rows(grad_conv))

    def branch_step(block, sums):
        main_sums, rest_sums = sums
        grads = []
        for base in (0, half):
            rows = rows_of(block, TALL, base)
            branch = dot_nt(cot_ref[rows], merge_ref[...]).astype(BF16)
            branch_s[rows] = branch
            grads.append(dot_nt(branch, down_ref[...]))
        for part in range(TALL // 64):
            inner = slice(part * 64, part * 64 + 64)
            start = block * TALL + part * 64
            for values, base in zip(grads, (0, half)):
                rows = chunk(start, base)
                gated, gate_pre, main_sums = branch_part(
                    values[inner, :LANES], rows, chunk(start, base + MARGIN), main_sums
                )
                mix_s[rows, :LANES] = gated.astype(BF16)
                gate_s[rows, :LANES] = gate_pre.astype(BF16)
            grad = jnp.where(low, grads[0][inner, LANES:], turn(grads[1][inner, LANES:]))
            gated, gate_pre, rest_sums = branch_part(
                grad, chunk(start, frames), chunk(start, frames + 3 * MARGIN), rest_sums
            )
            low_rows, high_rows = chunk(start), chunk(start, half)
            gate_s[low_rows, LANES:] = gate_pre.astype(BF16)
            gate_s[high_rows, LANES:] = turn(gate_pre).astype(BF16)
            mix_s[low_rows, LANES:] = jnp.where(low, gated, turn(attn_ref[low_rows])).astype(BF16)
            mix_s[high_rows, LANES:] = jnp.where(low, turn(gated), turn(attn_ref[high_rows])).astype(BF16)
        return main_sums, rest_sums

    (main_up, main_conv), (rest_up, rest_conv) = lax.fori_loop(
        0, half // TALL, branch_step, ((zero, zero), (zero, zero)), unroll=2
    )
    gate_pre_out.go()
    fill_margins(grad_s, frames)
    own = rows_of(place, BLOCK)
    lines_out[0:1] = one_row(fold_rows(branch_s[own].astype(F32)))
    lines_out[1:2] = one_row(fold_rows(cot_ref[own].astype(F32)))
    lines_out[2:8] = jnp.zeros((6, D), F32)
    grad_down = dot_tn(mix_s[...], branch_s[...])
    grad_gate = dot_tn(gate_s[...], n_ref[...])
    for quarter in range(quarters):
        for tile in range(4):
            early_out.buffer[quarter, tile * share : (tile + 1) * share] = grad_down[
                quarter * share : (quarter + 1) * share, tile * LANES : (tile + 1) * LANES
            ].astype(BF16)
        early_out.buffer[quarter, 4 * share :] = grad_gate[
            :channels, quarter * LANES : (quarter + 1) * LANES
        ].astype(BF16)
    early_out.go()
    for block in range(blocks):
        mixed_out.buffer[block, :BLOCK] = mix_s[block * BLOCK : (block + 1) * BLOCK]
    mixed_out.go(slice(None), pl.ds(0, BLOCK))

    def differentiate(step, limits):
        for index, base in enumerate(triple_places(step, frames)):
            forward_s[index] = conv_s[pl.ds(base, tall)]
            backward_s[index] = grad_s[pl.ds(base, tall)]
        for index in range(3):
            own = None if limits is None else limits[index]
            total = jnp.zeros((WINDOW // 8, 8, LANES), F32)
            centre = grouped(backward_s[index, MARGIN : MARGIN + WINDOW])
            for tap in range(KERNEL):
                mask = tap_mask(tap, own)
                total = total + tap_view(backward_s.at[index], tap, mask) * turn_s[index // 2, tap][None]
                tap_sum_s[index // 2, tap] += jnp.sum(tap_view(forward_s.at[index], tap, mask) * centre, axis=0)
            back_s[rows_of(step, WINDOW, outs[index])] = total.reshape(WINDOW, LANES)

    over_windows(bounds_s, frames, differentiate)
    lane = lax.broadcasted_iota(jnp.int32, (64, LANES), 1)

    def norm_part(rows, lines, sums):
        gain_sum, bias_sum = sums
        back, hat, slope = back_s[rows], hat_s[rows], slope_s[rows]
        grad = back * lines[2:3]
        grad_out.buffer[rows] = (grad * slope).astype(BF16)
        rate_out.buffer[rows] = slope.astype(BF16)
        along = back * hat
        return grad, along * lines[2:3], (gain_sum + fold_rows(along), bias_sum + fold_rows(back))

    def norm_step(block, sums):
        main_sums, rest_sums = sums
        for part in range(TALL // 64):
            start = block * TALL + part * 64
            pairs = []
            for base in (0, half):
                plain, along, main_sums = norm_part(chunk(start, base), main, main_sums)
                pairs.append([plain, along])
            plain, along, rest_sums = norm_part(chunk(start, frames), rest, rest_sums)
            for item, values in enumerate((plain, along)):
                pairs[0][item] = pairs[0][item] + jnp.where(low, values, 0.0)
                pairs[1][item] = pairs[1][item] + jnp.where(low, 0.0, values)
            for (plain, along), base in zip(pairs, (0, half)):
                columns_s[chunk(start, base)] = jnp.where(
                    lane == 0,
                    jnp.sum(plain, axis=-1, keepdims=True),
                    jnp.where(lane == 1, jnp.sum(along, axis=-1, keepdims=True), 0.0),
                )
        return main_sums, rest_sums

    (main_gain, main_bias), (rest_gain, rest_bias) = lax.fori_loop(
        0, half // TALL, norm_step, ((zero, zero), (zero, zero)), unroll=2
    )
    grad_out.go()
    rate_out.go()
    totals = jnp.concatenate(
        [jnp.transpose(columns_s[block * BLOCK : (block + 1) * BLOCK])[:2] for block in range(blocks)], axis=0
    )
    high = totals.astype(BF16)
    low_part = (totals - high.astype(F32)).astype(BF16)
    for block in range(blocks):
        mixed_out.buffer[block, BLOCK:, :LANES] = high
        mixed_out.buffer[block, BLOCK:, LANES:] = low_part
    mixed_out.go(slice(None), pl.ds(BLOCK, 2 * blocks))

    def vectors(part, lines):
        taps = jnp.sum(tap_sum_s[part], axis=1)[:KERNEL]
        stacked = jnp.concatenate([taps] + [one_row(line) for line in lines], axis=0)
        if part:
            stacked = stacked + turn(stacked)
        return jnp.transpose(
            jnp.concatenate([stacked, jnp.zeros((LANES - stacked.shape[0], LANES), F32)], axis=0)
        )

    vectors_out[:LANES] = vectors(0, (main_conv, main_gain, main_bias, main_up))
    vectors_out[LANES:] = vectors(1, (rest_conv, rest_gain, rest_bias, rest_up))[: channels - LANES]


def attend_back_kernel(
    cot_ref,
    merge_ref,
    head_ref,
    attn_ref,
    value_ref,
    prob_ref,
    key_ref,
    coarse_ref,
    fine_ref,
    pos_ref,
    query_ref,
    n_ref,
    q_position_ref,
    qkv_ref,
    hat_ref,
    gain_ref,
    early_ref,
    branch_out,
    total_out,
    pack_0,
    pack_1,
    pack_2,
    pack_3,
    lines_out,
    grad_s,
    raw_s,
    projected_s,
    parts_s,
    grads_s,
):
    place = lax.axis_index("tm")
    frames = raw_s.shape[0]
    blocks = frames // BLOCK
    half = D // 2
    zero = jnp.zeros((8, LANES), F32)
    cot_ref, merge_ref, head_ref, attn_ref = cot_ref(), merge_ref(), head_ref(), attn_ref()
    head_ref[HEAD:] = jnp.zeros((LANES - HEAD, D), BF16)
    begin(value_ref, prob_ref, key_ref, pos_ref)

    @pl.loop(0, frames // TALL, unroll=4)
    def _(block):
        rows = rows_of(block, TALL)
        branch = dot_nt(cot_ref[rows], merge_ref[...]).astype(BF16)
        branch_out.buffer[rows] = branch
        grad = (dot_nt(branch, head_ref[...]) * attn_ref[rows, HEAD : HEAD + 1]).astype(BF16).astype(F32)
        delta = jnp.sum(grad * attn_ref[rows], axis=1, keepdims=True)
        high = delta.astype(BF16).astype(F32)
        lane = lax.broadcasted_iota(jnp.int32, (TALL, LANES), 1)
        grad = jnp.where(lane == HEAD, -high, jnp.where(lane == HEAD + 1, high - delta, grad))
        grad_s[rows] = grad.astype(BF16)

    branch_out.go()
    value_ref, prob_ref = value_ref(), prob_ref()
    key_ref, pos_ref = key_ref(), pos_ref()
    begin(query_ref, n_ref, q_position_ref, qkv_ref, hat_ref, early_ref)

    def score_step(block, sums):
        content_sum, position_sum = sums
        rows = rows_of(block, TALL)
        grad = grad_s[rows]
        score = dot_nt(grad, value_ref[...])
        for part in range(TALL // 32):
            at = pl.ds(pl.multiple_of(block * TALL + part * 32, 32), 32)
            inner = slice(part * 32, part * 32 + 32)
            raw_s[at] = (prob_ref[at].astype(F32) * score[inner]).astype(BF16)
        query = dot_nn(raw_s[rows], key_ref[...]) * 0.125
        for part in range(TALL // 32):
            at = pl.ds(pl.multiple_of(block * TALL + part * 32, 32), 32)
            inner = part * 32 % BLOCK
            sine, cosine = angle_rows(
                coarse_ref, fine_ref, block * (TALL // BLOCK) + part * 32 // BLOCK, slice(inner, inner + 32)
            )
            inner = slice(part * 32, part * 32 + 32)
            first, second = query[inner, LANES : LANES + half], query[inner, LANES + half :]
            projected_s[at, :half] = (first * sine - second * cosine).astype(BF16)
            projected_s[at, half:] = (first * cosine + second * sine).astype(BF16)
        position = dot_nn(projected_s[rows], pos_ref[...])
        content = query[:, :LANES]
        parts_s[rows, :LANES] = (content + position).astype(BF16)
        return content_sum + fold_rows(content), position_sum + fold_rows(position)

    content_sum, position_sum = lax.fori_loop(0, frames // TALL, score_step, (zero, zero), unroll=4)
    query_ref, n_ref, q_position_ref = query_ref(), n_ref(), q_position_ref()
    qkv_ref, hat_ref = qkv_ref(), hat_ref()
    grad_key = dot_tn(query_ref[...], raw_s[...])
    grad_value = dot_tn(grad_s[...], prob_ref[...])
    for block in range(blocks):
        at = slice(block * BLOCK, (block + 1) * BLOCK)
        parts_s[at, LANES : 2 * LANES] = jnp.transpose(grad_key[:, at]).astype(BF16)
        parts_s[at, 2 * LANES :] = jnp.transpose(grad_value[:, at]).astype(BF16)
    grads_s[:HEAD] = dot_tn(parts_s[:, :LANES], n_ref[...])[:HEAD]
    grads_s[HEAD : 2 * HEAD] = dot_nn(grad_key.astype(BF16), n_ref[...])[:HEAD]
    grads_s[2 * HEAD : 3 * HEAD] = dot_nn(grad_value.astype(BF16), n_ref[...])[:HEAD]
    grads_s[3 * HEAD :] = dot_tn(q_position_ref[...], projected_s[...])[:HEAD]
    stream = lax.axis_index("stream")
    early_ref = early_ref()
    for apart, pack_out in enumerate((pack_0, pack_1, pack_2, pack_3)):
        quarter = lax.bitwise_xor(stream, jnp.int32(apart))
        lanes = pl.ds(pl.multiple_of(quarter * LANES, LANES), LANES)
        pack_out.buffer[: 4 * HEAD] = grads_s[:, lanes].astype(BF16)
        pack_out.buffer[4 * HEAD :] = early_ref[quarter]
        pack_out.go()
    gain = line_of(gain_ref)
    wide_zero = jnp.zeros((8, D), F32)

    def norm_step(block, sums):
        gain_sum, bias_sum = sums
        grad = dot_nt(parts_s[rows_of(block, TALL)], qkv_ref[...])
        for part in range(TALL // 32):
            at = pl.ds(pl.multiple_of(block * TALL + part * 32, 32), 32)
            own = grad[part * 32 : part * 32 + 32]
            total_out.buffer[at] = (own * gain).astype(BF16)
            gain_sum = gain_sum + fold_rows(own * hat_ref[at].astype(F32))
            bias_sum = bias_sum + fold_rows(own)
        return gain_sum, bias_sum

    gain_sum, bias_sum = lax.fori_loop(0, frames // TALL, norm_step, (wide_zero, wide_zero), unroll=4)
    lane = lax.broadcasted_iota(jnp.int32, (1, LANES), 1)

    def own_lanes(sums):
        line = one_row(sums)
        line = line + turn(line)
        tiles = [
            jnp.where(lax.div(tile * LANES + lane, HEAD) == place, line, 0.0) for tile in range(D // LANES)
        ]
        return jnp.concatenate(tiles, axis=1)

    lines_out[...] = jnp.concatenate(
        [
            one_row(gain_sum),
            one_row(bias_sum),
            own_lanes(content_sum),
            own_lanes(position_sum),
            jnp.zeros((4, D), F32),
        ],
        axis=0,
    )


def mlp_second_kernel(
    mixed_ref,
    gate_pre_ref,
    grad_ref,
    rate_ref,
    hat_ref,
    up_ref,
    norm_hat_ref,
    gain_ref,
    other_ref,
    pre_out,
    same_out,
    apart_out,
    lines_out,
    up_out,
    columns_s,
):
    place = lax.axis_index("tm")
    pre_s = pre_out.buffer
    frames = pre_s.shape[0]
    half = frames // 2
    blocks = frames // BLOCK
    totals = jnp.zeros((2 * blocks, LANES), F32)
    mixed_ref = mixed_ref()
    for source in range(mixed_ref.shape[0]):
        both = mixed_ref[source].astype(F32)
        totals = totals + (both[:, :LANES] + both[:, LANES:])
    totals = totals * (1.0 / HALF)
    high = totals.astype(BF16)
    low_part = (totals - high.astype(F32)).astype(BF16)
    both = jnp.concatenate([high, low_part], axis=0)
    lane = lax.broadcasted_iota(jnp.int32, (4 * blocks, 2 * LANES), 1) // LANES
    line = lax.broadcasted_iota(jnp.int32, (4 * blocks, 2 * LANES), 0)
    for block in range(blocks):
        chosen = (lax.rem(line, 2 * blocks) == 2 * block + lane).astype(F32).astype(BF16)
        columns_s[block * BLOCK : (block + 1) * BLOCK] = dot_tn(both, chosen)
    gate_pre_ref, grad_ref, rate_ref, hat_ref = gate_pre_ref(), grad_ref(), rate_ref(), hat_ref()
    begin(up_ref, norm_hat_ref, other_ref)
    low = low_lanes(64)
    gain = line_of(gain_ref)

    def chunk(start, base=0):
        return pl.ds(pl.multiple_of(start, 64) + base, 64)

    def pre_part(rows, table, up_sum):
        plain, along = table
        hat, rate = hat_ref[rows].astype(F32), rate_ref[rows].astype(F32)
        pre = (grad_ref[rows].astype(F32) - rate * (plain + hat * along)).astype(BF16).astype(F32)
        return pre, up_sum + fold_rows(pre)

    def pre_step(block, sums):
        main_up, rest_up = sums
        for part in range(TALL // 64):
            start = block * TALL + part * 64
            tables = []
            for base in (0, half):
                rows = chunk(start, base)
                table = [columns_s[rows, item * LANES : (item + 1) * LANES] for item in range(2)]
                tables.append(table)
                pre, main_up = pre_part(rows, table, main_up)
                pre_s[rows, :LANES] = gate_pre_ref[rows]
                pre_s[rows, 2 * LANES :] = pre.astype(BF16)
            rows = chunk(start, frames)
            table = [jnp.where(low, one, other) for one, other in zip(*tables)]
            pre, rest_up = pre_part(rows, table, rest_up)
            gate_pre = gate_pre_ref[rows].astype(F32)
            pre_s[chunk(start), LANES : 2 * LANES] = jnp.where(low, gate_pre, turn(pre)).astype(BF16)
            pre_s[chunk(start, half), LANES : 2 * LANES] = jnp.where(low, turn(gate_pre), pre).astype(BF16)
        return main_up, rest_up

    zero = jnp.zeros((8, LANES), F32)
    main_up, rest_up = lax.fori_loop(0, half // TALL, pre_step, (zero, zero), unroll=2)
    pre_out.go()
    up_ref, norm_hat_ref, other_ref = up_ref(), norm_hat_ref(), other_ref()
    wide_zero = jnp.zeros((8, D), F32)

    def norm_step(step, sums):
        gain_sum, bias_sum = sums
        grads = dot_nt(pre_s[rows_of(step, TALL)], up_ref[...])
        for part in range(TALL // BLOCK):
            block = step * (TALL // BLOCK) + part
            rows = rows_of(block, BLOCK)
            grad = grads[part * BLOCK : (part + 1) * BLOCK]
            total = (grad * gain + other_ref[rows].astype(F32)).astype(BF16)
            apart = lax.bitwise_xor(block, place)

            @pl.when(lax.rem(apart, 2) == 0)
            def _(apart=apart, total=total):
                same_out.buffer[lax.div(apart, 2)] = total

            @pl.when(lax.rem(apart, 2) == 1)
            def _(apart=apart, total=total):
                apart_out.buffer[lax.div(apart, 2)] = total

            gain_sum = gain_sum + fold_rows(grad * norm_hat_ref[rows].astype(F32))
            bias_sum = bias_sum + fold_rows(grad)
        return gain_sum, bias_sum

    gain_sum, bias_sum = lax.fori_loop(0, frames // TALL, norm_step, (wide_zero, wide_zero), unroll=2)
    apart_out.go()
    same_out.go()
    lines_out[...] = jnp.concatenate([one_row(gain_sum), one_row(bias_sum), jnp.zeros((6, D), F32)], axis=0)
    rest_line = one_row(rest_up)
    up_out[:LANES] = jnp.transpose(jnp.broadcast_to(one_row(main_up), (LANES, LANES)))
    up_out[LANES:] = jnp.transpose(jnp.broadcast_to(rest_line + turn(rest_line), (LANES, LANES)))[:LOW]


def late_pack_kernel(
    pre_ref,
    n_ref,
    joined_ref,
    branch_ref,
    cot_ref,
    vectors_ref,
    up_columns_ref,
    first_lines_ref,
    head_lines_ref,
    own_lines_ref,
    pack_out,
):
    pack_ref = pack_out.buffer
    quarters = pack_ref.shape[0]
    channels = vectors_ref.shape[0]
    share = channels // quarters
    gate_at = KERNEL + 3
    lane = lax.broadcasted_iota(jnp.int32, (share, LANES), 1)
    lines = jnp.concatenate(
        [
            head_lines_ref[0:2],
            own_lines_ref[0:2],
            head_lines_ref[2:4],
            first_lines_ref[0:2],
            jnp.zeros((8, D), F32),
        ],
        axis=0,
    )
    for quarter in range(quarters):
        table = vectors_ref[quarter * share : (quarter + 1) * share]
        for other in range(2):
            at = slice((2 * (quarter % 2) + other) * share, (2 * (quarter % 2) + other + 1) * share)
            column = vectors_ref[at, gate_at : gate_at + 1] if quarter < quarters // 2 else up_columns_ref[at, 0:1]
            table = jnp.where(lane == gate_at + other, column, table)
        pack_ref[quarter, channels : channels + share] = table.astype(BF16)
        pack_ref[quarter, channels + share : channels + share + 16] = lines[
            :, quarter * LANES : (quarter + 1) * LANES
        ].astype(BF16)
    grad_up = dot_tn(pre_ref()[...], n_ref()[...])
    for quarter in range(quarters):
        lanes = slice(quarter * LANES, (quarter + 1) * LANES)
        pack_ref[quarter, :LANES] = grad_up[LANES:, lanes].astype(BF16)
        pack_ref[quarter, LANES:channels] = grad_up[LOW:LANES, lanes].astype(BF16)
    joined_ref, cot_ref, branch_ref = joined_ref(), cot_ref(), branch_ref()
    sources, _, rows = joined_ref.shape
    merge_rows = 2 * D // sources
    head_rows = D // sources
    grad_merge = jnp.zeros((merge_rows, D), F32)
    grad_head = jnp.zeros((head_rows, D), F32)
    for source in range(sources):
        at = slice(source * rows, (source + 1) * rows)
        joined = joined_ref[source]
        grad_merge = grad_merge + dot_nn(joined[:merge_rows], cot_ref[at])
        grad_head = grad_head + dot_nn(joined[merge_rows : merge_rows + head_rows], branch_ref[at])
    for quarter in range(quarters):
        base = channels + share + 16
        for grad in (grad_merge, grad_head):
            part = grad.shape[0] // quarters
            for tile in range(4):
                pack_ref[quarter, base : base + part] = grad[
                    quarter * part : (quarter + 1) * part, tile * LANES : (tile + 1) * LANES
                ].astype(BF16)
                base += part


def output_kernel(
    x_ref, mixed_ref, head_ref, down_ref, down_bias_ref, merge_ref, merge_bias_ref, out_ref, joined_out
):
    sources = mixed_ref.shape[0]
    rows = x_ref.shape[0]
    channels = HALF // sources
    share = channels // 4
    attn_parts = []
    branch_attn = jnp.zeros((rows, D), F32)
    branch_mlp = jnp.zeros((rows, D), F32)
    for source in range(sources):
        attn = turn(mixed_ref[source, :rows, LANES:].astype(F32))[:, :HEAD].astype(BF16)
        attn_parts.append(attn)
        branch_attn = branch_attn + dot_nn(attn, head_ref[source * HEAD : (source + 1) * HEAD])
        down = jnp.concatenate(
            [down_ref[(part * sources + source) * share : (part * sources + source + 1) * share] for part in range(4)],
            axis=0,
        )
        branch_mlp = branch_mlp + dot_nn(mixed_ref[source, :rows, :channels], down)
    joined = jnp.concatenate(
        [branch_attn.astype(BF16), (branch_mlp + line_of(down_bias_ref)).astype(BF16)], axis=1
    )
    result = x_ref[...].astype(F32) + dot_nn(joined, merge_ref[...]) + line_of(merge_bias_ref)
    out_ref[...] = result.astype(BF16)
    turned = jnp.transpose(joined.astype(F32))
    heads = jnp.transpose(jnp.concatenate(attn_parts, axis=1).astype(F32))
    merge_share = turned.shape[0] // (4 * sources)
    head_share = heads.shape[0] // (4 * sources)
    used = 4 * (merge_share + head_share)
    for target in range(sources):
        for part in range(4):
            at = (part * sources + target) * merge_share
            joined_out[target, part * merge_share : (part + 1) * merge_share] = turned[
                at : at + merge_share
            ].astype(BF16)
            at = (part * sources + target) * head_share
            to = 4 * merge_share + part * head_share
            joined_out[target, to : to + head_share] = heads[at : at + head_share].astype(BF16)
        joined_out[target, used:] = jnp.zeros((joined_out.shape[1] - used, rows), BF16)


def pair_kernel(same_ref, other_ref, *out_refs):
    for slot, out_ref in enumerate(out_refs):
        out_ref[...] = (same_ref[slot].astype(F32) + other_ref[slot].astype(F32)).astype(BF16)


def frames_kernel(x_ref, cot_ref, *refs):
    total_refs, out_ref = refs[:-1], refs[-1]
    for part in range(x_ref.shape[0] // 32):
        rows = slice(part * 32, part * 32 + 32)
        inputs = x_ref[rows].astype(F32)
        mean = jnp.mean(inputs, axis=-1, keepdims=True)
        centred = inputs - mean
        rate = lax.rsqrt(jnp.mean(centred * centred, axis=-1, keepdims=True) + EPS)
        hat = centred * rate
        grad = total_refs[0][rows].astype(F32)
        for total_ref in total_refs[1:]:
            grad = grad + total_ref[rows].astype(F32)
        plain = jnp.mean(grad, axis=-1, keepdims=True)
        along = jnp.mean(grad * hat, axis=-1, keepdims=True)
        out_ref[rows] = cot_ref[rows].astype(F32) + rate * (grad - plain - hat * along)


def add_kernel(*refs):
    out_ref = refs[-1]
    first = 0
    for at in range(0, len(refs) - 1, 4):
        total = refs[at][...].astype(F32)
        for ref in refs[at + 1 : at + 4]:
            total = total + ref[...].astype(F32)
        out_ref[first : first + total.shape[0]] = total.astype(BF16)
        first += total.shape[0]


def gather_parts(near_ref, far_ref, all_s):
    place = lax.axis_index("tm")
    for apart in range(all_s.shape[0]):
        part_ref = far_ref if apart % 2 else near_ref
        all_s[lax.bitwise_xor(jnp.int32(apart), place)] = part_ref[apart // 2]


def lines_from(all_s, base, size):
    return jnp.concatenate([all_s[source, base : base + size] for source in range(all_s.shape[0])], axis=0).astype(F32)


def add_streams_kernel(parts_ref, out_ref):
    total = parts_ref[0].astype(F32)
    for source in range(1, parts_ref.shape[0]):
        total = total + parts_ref[source].astype(F32)
    out_ref[...] = total.astype(BF16)


def early_kernel(near_ref, far_ref, qkv_out, pos_out, down_out, up_out, all_s):
    gather_parts(near_ref, far_ref, all_s)
    sources = all_s.shape[0]
    share = HALF // (4 * sources)
    for kind in range(4):
        lines = jnp.transpose(lines_from(all_s, kind * HEAD, HEAD))
        if kind < 3:
            qkv_out[:, kind * D : (kind + 1) * D] = lines
        else:
            pos_out[...] = lines
    base = 4 * HEAD
    for source in range(sources):
        for tile in range(4):
            down_out[source * share : (source + 1) * share, tile * LANES : (tile + 1) * LANES] = all_s[
                source, base + tile * share : base + (tile + 1) * share
            ].astype(F32)
    wide = sources * share
    for group in range(4):
        up_out.buffer[:, group * wide : (group + 1) * wide] = jnp.transpose(
            lines_from(all_s, base + 4 * share + group * share, share)
        )


def late_kernel(*refs):
    _, near_ref, far_ref = refs[:3]
    (
        attn_gain_out,
        attn_bias_out,
        mlp_gain_out,
        mlp_bias_out,
        content_out,
        position_out,
        outw_out,
        up_out,
        up_bias_out,
        gain_out,
        bias_out,
        taps_out,
        conv_bias_out,
        down_bias_out,
        merge_out,
        merge_bias_out,
        all_s,
    ) = refs[3:]
    gather_parts(near_ref, far_ref, all_s)
    sources = all_s.shape[0]
    channels = HALF // sources
    share = channels // 4
    base = 0
    for group in range(4):
        at = group * sources * share
        up_out.buffer[:, at : at + sources * share] = jnp.transpose(lines_from(all_s, base + group * share, share))
    up_out.go()
    table = jnp.transpose(lines_from(all_s, base + channels, share))
    taps_out[...] = table[:KERNEL]
    conv_bias_out[...] = table[KERNEL]
    gain_out[...] = table[KERNEL + 1]
    bias_out[...] = table[KERNEL + 2]
    wide = sources * share
    up_bias_out[:wide] = table[KERNEL + 3]
    up_bias_out[wide:] = table[KERNEL + 4]
    base = base + channels + share
    lines = all_s[0, base : base + 16].astype(F32)
    for source in range(1, sources):
        lines = lines + all_s[source, base : base + 16].astype(F32)
    outs = (attn_gain_out, attn_bias_out, mlp_gain_out, mlp_bias_out, content_out, position_out, down_bias_out, merge_bias_out)
    for line, out in enumerate(outs):
        out[...] = lines[line]
    base = base + 16
    merge_share = 2 * D // (4 * sources)
    head_share = D // (4 * sources)
    for source in range(sources):
        for tile in range(4):
            lanes = slice(tile * LANES, (tile + 1) * LANES)
            at = base + tile * merge_share
            merge_out[source * merge_share : (source + 1) * merge_share, lanes] = all_s[
                source, at : at + merge_share
            ].astype(F32)
            at = base + 4 * merge_share + tile * head_share
            outw_out[source * head_share : (source + 1) * head_share, lanes] = all_s[
                source, at : at + head_share
            ].astype(F32)


def moved(block, axis, bits):
    count = lax.axis_size(axis)
    return lax.ppermute(block, axis, [(index, index ^ bits) for index in range(count)])


def over_streams(packs):
    return [packs[0]] + [moved(packs[bits], "stream", bits) for bits in range(1, lax.axis_size("stream"))]


def near_blocks(block):
    return [block] + [moved(block, "tm", bits) for bits in range(2, lax.axis_size("tm"), 2)]


def far_blocks(near):
    far = [moved(part, "tm", 1) for part in near]
    return [part for pair in zip(near, far) for part in pair]


def far_stack(near):
    stack = jnp.stack(near)
    return stack, moved(stack, "tm", 1)


def head_device(
    frames,
    lengths,
    cotangent,
    ln_attn_gain,
    ln_attn_bias,
    ln_mlp_gain,
    ln_mlp_bias,
    qkv_weight,
    content_bias,
    position_bias,
    pos_weight,
    out_weight,
    up_weight,
    up_bias,
    gate_norm_gain,
    gate_norm_bias,
    conv_kernel,
    conv_bias,
    down_weight,
    down_bias,
    merge_weight,
    merge_bias,
):
    count = lax.axis_size("tm")
    quarters = lax.axis_size("stream")
    own = frames.shape[1]
    total = own * count
    folded = total + total // 2
    padded = folded + 4 * MARGIN
    share = HALF // (quarters * count)
    channels = HALF // count
    quarter = D // quarters
    own_frames = frames[0]
    own_cotangent = cotangent[0]

    whole, late = Part(), Part(late=True)
    near = near_blocks(jnp.concatenate([own_frames, own_cotangent], axis=1))
    up_own, table, qkv_own, pos_own, bias_own = kernel_call(
        select_kernel,
        [
            ((D, 3 * LANES), BF16),
            ((2, 8 + KERNEL + 1, LANES), F32),
            ((D, 3 * LANES), BF16),
            ((D, LANES), BF16),
            ((8, LANES), F32),
        ],
        10 * "v",
    )(
        up_weight,
        up_bias,
        gate_norm_gain,
        gate_norm_bias,
        conv_bias,
        conv_kernel,
        qkv_weight,
        pos_weight,
        content_bias,
        position_bias,
    )
    frequency = jnp.exp(jnp.arange(D // 2, dtype=F32) * (-2.0 * math.log(10000.0) / D))
    coarse = jnp.arange(0, total, BLOCK, dtype=F32)[:, None] * frequency[None]
    fine = jnp.arange(BLOCK, dtype=F32)[:, None] * frequency[None]
    coarse_table = jnp.concatenate([jnp.sin(coarse), jnp.cos(coarse)], axis=1)
    fine_table = jnp.concatenate([jnp.sin(fine), jnp.cos(fine)], axis=1)
    near, up_own, coarse_table, fine_table = lax.optimization_barrier((near, up_own, coarse_table, fine_table))
    blocks = far_blocks(near)

    n_attn, n_mlp, hat, q_position, query, key, value, prob, attn, mean, rate = kernel_call(
        attend_kernel,
        [
            ((total, D), BF16, 1),
            ((total, D), BF16, 1),
            ((total, D), BF16, 1),
            ((total, LANES), BF16, 1),
            ((total, LANES + D), BF16, 1),
            ((total, LANES + D), BF16, 1),
            ((total, LANES), BF16, 1),
            ((total, total), BF16, 1),
            ((total, LANES), F32, 1),
            ((total, LANES), F32, 1),
            ((total, LANES), F32, 1),
        ],
        [
            "s",
            blocks_part(0),
            *"vvvvvvvvv",
            Part((D, HALF), lambda refs, buffer: [(refs[0].at[:, pl.ds(HALF, HALF)], buffer)], late=True),
            "v",
        ],
        bounds=True,
    )(
        lengths,
        *blocks,
        ln_attn_gain,
        ln_attn_bias,
        ln_mlp_gain,
        ln_mlp_bias,
        qkv_own,
        pos_own,
        bias_own,
        coarse_table,
        fine_table,
        up_weight,
        up_bias,
    )

    def own_down(refs, buffer):
        place = lax.axis_index("tm")
        stride = HALF // quarters
        return [
            (
                refs[0].at[pl.ds(pl.multiple_of(part * stride + share * place, 16), share)],
                buffer.at[pl.ds(part * share, share)],
            )
            for part in range(quarters)
        ]

    mixed, gate_pre, grad_y, slope, gate_hat, early_pack, vectors, first_lines = kernel_call(
        mlp_first_kernel,
        [
            ((count, own + 16, 2 * LANES), BF16, 1),
            ((folded, LANES), BF16, 1),
            ((folded, LANES), BF16, 1),
            ((folded, LANES), BF16, 1),
            ((folded, LANES), BF16, 1),
            ((quarters, 8 * share, LANES), BF16, 1),
            ((channels, LANES), F32),
            ((8, D), F32),
        ],
        [
            "s",
            whole,
            "v",
            "v",
            whole,
            whole,
            blocks_part(1, late=True),
            rows_part(D, D, late=True),
            Part((2 * LANES, D), own_down, late=True),
            Part(late=True),
        ],
        [
            ((folded, LANES), F32),
            ((folded, LANES), F32),
            ((total, 2 * LANES), BF16),
            ((folded, LANES), F32),
            ((folded, LANES), F32),
            ((padded, LANES), F32),
            ((padded, LANES), F32),
            ((folded, LANES), F32),
            ((folded, LANES), F32),
            ((total, D), BF16),
            ((total, 2 * LANES), BF16),
            ((2, 32, 8, LANES), F32),
            ((2, 32, 8, LANES), F32),
            ((2, 32, 8, LANES), F32),
            ((total, LANES), F32),
            ((3, WINDOW + 2 * MARGIN, LANES), F32),
            ((3, WINDOW + 2 * MARGIN, LANES), F32),
        ],
        bounds=True,
    )(lengths, n_mlp, up_own, table, mean, rate, *blocks, merge_weight, down_weight, attn)
    mixed_own = lax.all_to_all(mixed, "tm", 0, 0, tiled=True)

    def own_head(refs, buffer):
        at = pl.ds(pl.multiple_of(lax.axis_index("tm") * HEAD, HEAD), HEAD)
        return [(refs[0].at[at], buffer.at[pl.ds(0, HEAD)])]

    branch, from_attn, *head_packs, head_lines = kernel_call(
        attend_back_kernel,
        [
            ((total, D), BF16, 1),
            ((total, D), BF16, 1),
            *([((4 * HEAD + 8 * share, LANES), BF16, 1)] * quarters),
            ((8, D), F32),
        ],
        [
            blocks_part(1),
            rows_part(0, D),
            Part((LANES, D), own_head),
            whole,
            late,
            late,
            late,
            "v",
            "v",
            late,
            Part((total, LANES), lambda refs, buffer: [(refs[0].at[:, pl.ds(0, LANES)], buffer)], late=True),
            late,
            late,
            late,
            late,
            "v",
            late,
        ],
        [
            ((total, LANES), BF16),
            ((total, total), BF16),
            ((total, D), BF16),
            ((total, 3 * LANES), BF16),
            ((4 * HEAD, D), F32),
        ],
    )(
        *blocks,
        merge_weight,
        out_weight,
        attn,
        value,
        prob,
        key,
        coarse_table,
        fine_table,
        pos_own,
        query,
        n_attn,
        q_position,
        qkv_own,
        hat,
        ln_attn_gain,
        early_pack,
    )
    head_parts = over_streams(head_packs)
    mixed_own, _ = lax.optimization_barrier((mixed_own, head_lines))
    out_rows, joined = kernel_call(
        output_kernel,
        [((own, D), BF16), ((count, 256, own), BF16)],
        "vvvvvvv",
        megas=24,
    )(own_frames, mixed_own, out_weight, down_weight, down_bias, merge_weight, merge_bias)
    joined_all = lax.all_to_all(joined, "tm", 0, 0, tiled=True)
    gate_pre, _ = lax.optimization_barrier((gate_pre, joined))
    late_rows = 5 * share + 16 + 3 * D // count
    pre, same, apart, own_lines, up_columns = kernel_call(
        mlp_second_kernel,
        [
            ((total, 3 * LANES), BF16, 1),
            ((count // 2, own, D), BF16, 1),
            ((count // 2, own, D), BF16, 1),
            ((8, D), F32),
            ((channels, LANES), F32),
        ],
        [
            Part(
                (count, 2 * total // BLOCK, 2 * LANES),
                lambda refs, buffer: [(refs[0].at[:, pl.ds(own, 2 * total // BLOCK)], buffer)],
            ),
            *([whole] * 4),
            late,
            late,
            "v",
            late,
        ],
        [((total, 2 * LANES), F32)],
    )(mixed_own, gate_pre, grad_y, slope, gate_hat, up_own, hat, ln_mlp_gain, from_attn)
    sibling = moved(apart, "tm", 1)
    pre, joined_all = lax.optimization_barrier((pre, joined_all))
    (late_pack,) = kernel_call(
        late_pack_kernel,
        [((quarters, late_rows, LANES), BF16, 1)],
        [
            Part(
                (total, 2 * LANES),
                lambda refs, buffer: [(refs[0].at[:, pl.ds(LANES, 2 * LANES)], buffer)],
            ),
            whole,
            whole,
            whole,
            blocks_part(1),
            *"vvvvv",
        ],
    )(pre, n_mlp, joined_all, branch, *blocks, vectors, up_columns, first_lines, head_lines, own_lines)
    late_pack, head_parts = lax.optimization_barrier((late_pack, head_parts))
    late_moved = lax.all_to_all(late_pack, "stream", 0, 0, tiled=True)
    (early_part,) = kernel_call(add_kernel, [((4 * HEAD + 8 * share, LANES), BF16)], quarters * "v", megas=24)(
        *head_parts
    )
    early_near = near_blocks(early_part)
    pairs = kernel_call(pair_kernel, [((own, D), BF16)] * (count // 2), "vv", megas=24)(same, sibling)
    sums = [pairs[0]] + [moved(pairs[slot], "tm", 2 * slot) for slot in range(1, count // 2)]
    late_moved, early_near, sums = lax.optimization_barrier((late_moved, early_near, sums))
    (late_part,) = kernel_call(add_streams_kernel, [((late_rows, LANES), BF16)], "v", megas=24)(late_moved)
    late_near = near_blocks(late_part)
    early_all = far_stack(early_near)
    grad_qkv, grad_pos, grad_down, half_up = kernel_call(
        early_kernel,
        [
            ((quarter, 3 * D), F32),
            ((quarter, D), F32),
            ((HALF // quarters, D), F32),
            ((quarter, 2 * HALF), F32, 1, (quarter, HALF), lambda ref: ref.at[:, pl.ds(0, HALF)]),
        ],
        "vv",
        [((count, 4 * HEAD + 8 * share, LANES), BF16)],
        megas=24,
    )(*early_all)
    late_near, grad_pos, sums = lax.optimization_barrier((late_near, grad_pos, sums))
    late_parts = far_stack(late_near)
    (grad_frames,) = kernel_call(frames_kernel, [((own, D), F32)], (2 + count // 2) * "v", megas=24)(
        own_frames, own_cotangent, *sums
    )
    late_parts, grad_frames = lax.optimization_barrier((late_parts, grad_frames))
    late = kernel_call(
        late_kernel,
        [((quarter,), F32)] * 6
        + [
            ((quarter, D), F32),
            ((quarter, 2 * HALF), F32, 1, (quarter, HALF), lambda ref: ref.at[:, pl.ds(HALF, HALF)]),
            ((2 * HALF // quarters,), F32),
            ((HALF // quarters,), F32),
            ((HALF // quarters,), F32),
            ((KERNEL, HALF // quarters), F32),
            ((HALF // quarters,), F32),
            ((quarter,), F32),
            ((2 * D // quarters, D), F32),
            ((quarter,), F32),
        ],
        "kvv",
        [((count,) + late_part.shape, BF16)],
        megas=24,
        aliases={0: 7},
    )(half_up, *late_parts)
    return (
        out_rows[None],
        grad_frames[None],
        *late[:4],
        grad_qkv,
        *late[4:6],
        grad_pos,
        *late[6:13],
        grad_down,
        *late[13:],
    )


def per_device(*operands):
    fits = (
        lax.axis_size("tm") == HEADS
        and lax.axis_size("stream") * LANES == D
        and operands[0].shape[1] == BLOCK
    )
    return head_device(*operands) if fits else frame_device(*operands)


def solution(mesh):
    return jax.shard_map(
        per_device,
        mesh=mesh,
        in_specs=(
            P("stream", "tm", None),
            P("stream", None),
            P("stream", "tm", None),
            P(),
            P(),
            P(),
            P(),
            P(),
            P(),
            P(),
            P(),
            P(),
            P(),
            P(),
            P(),
            P(),
            P(),
            P(),
            P(),
            P(),
            P(),
            P(),
        ),
        out_specs=(
            P("stream", "tm", None),
            P("stream", "tm", None),
            P("stream"),
            P("stream"),
            P("stream"),
            P("stream"),
            P("stream", None),
            P("stream"),
            P("stream"),
            P("stream", None),
            P("stream", None),
            P("stream", None),
            P("stream"),
            P("stream"),
            P("stream"),
            P(None, "stream"),
            P("stream"),
            P("stream", None),
            P("stream"),
            P("stream", None),
            P("stream"),
        ),
        check_vma=False,
    )
```
